32 devices in a mesh: dp: 8 (over z, y), tensor: 4 (over x, core).
Axes of the slice: x: 2, y: 2, z: 4, core: 2. Of those that a mesh axis runs over, the one named last changes fastest.
Arguments:
- tokens: bfloat16 [32768, 768], P('dp'), may hold values from -6 to 6
- lengths: int32 [32], P('dp'), may hold values from 128 to 1024, as said below
- tie_map: int32 [4], replicated, may hold values from 0 to 3, as said below
- norm_gains: bfloat16 [4, 2, 768], P(None, None, ('dp', 'tensor')), may hold values from 0.25 to 1.75
- bias_rows: bfloat16 [4, 10, 768], P(None, None, ('dp', 'tensor')), may hold values from -2 to 2
- attention_in: bfloat16 [4, 3, 768, 768], P(None, None, 'dp', 'tensor'), may hold values from -0.3125 to 0.3125
- attention_out: bfloat16 [4, 768, 768], P(None, 'tensor', 'dp'), may hold values from -0.875 to 0.875
- expand_weight: bfloat16 [4, 768, 3072], P(None, 'dp', 'tensor'), may hold values from -0.21875 to 0.21875
- project_weight: bfloat16 [4, 3072, 768], P(None, 'tensor', 'dp'), may hold values from -0.109375 to 0.109375
- cotangent: bfloat16 [32768, 768], P('dp'), may hold values from -6 to 6
Outputs:
- layer_out: bfloat16 [32768, 768], P('dp')
- tokens_grad: bfloat16 [32768, 768], P('dp')
- gains_grad: float32 [4, 2, 768], P(None, None, ('dp', 'tensor'))
- bias_grad: float32 [4, 10, 768], P(None, None, ('dp', 'tensor'))
- attention_in_grad: float32 [4, 3, 768, 768], P(None, None, 'dp', 'tensor')
- attention_out_grad: float32 [4, 768, 768], P(None, 'tensor', 'dp')
- expand_grad: float32 [4, 768, 3072], P(None, 'dp', 'tensor')
- project_grad: float32 [4, 3072, 768], P(None, 'tensor', 'dp')
The draws below stay inside these ranges and needn't reach their ends.
Inputs may be any that keep to these rules, and one draw needn't show every extreme that they name: `lengths`: the live tokens of a slot come first in it, the rest is padding. `tie_map`: kind 0: first norm, query, key and value projections with their biases; kind 1: attention output projection and bias; kind 2: second norm, first feed-forward matrix and bias; kind 3: second feed-forward matrix and bias. Every source is named by some kind.
All inputs are finite; a program needn't handle non-finite values.
Results may differ from the reference program's by a relative error of at most 0.019.
Values may be sent and summed in bfloat16 or wider, within the bound.
A program may use at most 192 MiB of HBM per device.

```python
import math
import jax
import jax.numpy as jnp
from jax import lax

D = 768
HEADS = 12
HEAD_DIM = 64
FF = 3072
SLOT_LEN = 1024
MIN_LEN = 128
NSRC = 4
SLOT_DEV = 4
BROWS = 10
SLOTS = 32
TOKENS = 32768
N_DP = 8
N_TENSOR = 4


def draw_lengths(key, part):
    key = jax.random.fold_in(key, 11)
    first_key, second_key = jax.random.split(key)
    drawn = jax.random.randint(first_key, (SLOTS,), MIN_LEN, SLOT_LEN + 1)
    longest = jax.random.randint(second_key, (), 0, SLOTS)
    places = jnp.arange(SLOTS)
    drawn = jnp.where(places == longest, SLOT_LEN, drawn)
    drawn = jnp.where(places == (longest + 1) % SLOTS, MIN_LEN, drawn)
    return drawn.astype(jnp.int32)


def draw_tie_map(key, part):
    key = jax.random.fold_in(key, 23)
    first_key, second_key = jax.random.split(key)
    leading = jax.random.permutation(first_key, NSRC).astype(jnp.int32)
    extra = 4 - NSRC
    if extra > 0:
        trailing = jax.random.randint(second_key, (extra,), 0, NSRC).astype(jnp.int32)
        return jnp.concatenate([leading, trailing]).astype(jnp.int32)
    return leading


def spiked(result, key, source, target, parts, factor):
    def block_of(dim):
        return (jnp.arange(result.shape[dim]) // (result.shape[dim] // parts)).reshape((-1,) + (1,) * (result.ndim - 1 - dim))

    near = jax.random.permutation(key, parts)[block_of(target)]
    second = (block_of(target) + parts // 2) % parts
    return jnp.where((block_of(source) == near) | (block_of(source) == second), factor * result, result)


def steps_of(own_key, extent, cuts, smallest, top_value):
    def one(dim, blocks):
        draws = jax.random.uniform(jax.random.fold_in(jax.random.fold_in(own_key, 6), dim), (blocks,), jnp.float32, smallest / len(cuts), top_value / len(cuts))
        return jnp.repeat(jnp.exp(draws), extent[dim] // blocks).reshape((-1,) + (1,) * (len(extent) - dim - 1))

    gain = one(*cuts[0])
    for cut in cuts[1:]:
        gain = gain * one(*cut)
    return gain


def centred(stream_key, shape, spread, bound, cuts=(), kind=jnp.bfloat16):
    factor_of = steps_of(stream_key, shape, cuts, -0.22, 0.18) if cuts else 1.0
    result = jax.random.normal(stream_key, shape, jnp.float32) * spread * factor_of
    return jnp.minimum(jnp.maximum(result, -bound), bound).astype(kind)


def gaussian_with(rng, shape, deviation, reach, cuts, heavy, kind=jnp.bfloat16):
    entries = deviation * jax.random.normal(rng, shape, jnp.float32)
    if cuts:
        entries = entries * steps_of(rng, shape, cuts, -0.22, 0.18)
    return jnp.clip(spiked(entries, jax.random.fold_in(rng, 3), *heavy), -reach, reach).astype(kind)


def setup_inputs(seed: int = 0) -> dict:
    arg_keys = jax.random.split(jax.random.key(seed), 11)
    return {
        "tokens": centred(arg_keys[0], (TOKENS, D), 1.0, 6.0, ((0, 8),)),
        "lengths": draw_lengths(jax.random.fold_in(arg_keys[10], 71), 0),
        "tie_map": draw_tie_map(jax.random.fold_in(arg_keys[10], 71), 0),
        "norm_gains": jnp.clip(1.0 + 0.15 * jax.random.normal(arg_keys[3], (NSRC, 2, D), jnp.float32), 0.25, 1.75).astype(jnp.bfloat16),
        "bias_rows": centred(arg_keys[4], (NSRC, BROWS, D), 0.3, 2.0, ((2, 32),)),
        "attention_in": centred(arg_keys[5], (NSRC, 3, D, D), (D // 2) ** -0.5, 0.3125, ((2, 8), (3, 4))),
        "attention_out": centred(arg_keys[6], (NSRC, D, D), (D // 16) ** -0.5, 0.875, ((1, 4), (2, 8))),
        "expand_weight": centred(arg_keys[7], (NSRC, D, FF), D ** -0.5, 0.21875, ((1, 8), (2, 4))),
        "project_weight": centred(arg_keys[8], (NSRC, FF, D), FF ** -0.5, 0.109375, ((1, 4), (2, 8))),
        "cotangent": gaussian_with(arg_keys[9], (TOKENS, D), 1.0, 6.0, ((0, 8),), (0, 1, 8, 2.0)),
    }


@jax.custom_vjp
def low(v):
    return lax.optimization_barrier(v.astype(jnp.bfloat16)).astype(jnp.float32)

@jax.custom_vjp
def low_back(v):
    return v

def low_keep(v):
    return (low(v), None)

def low_pass(kept, grad):
    return (grad,)

def back_keep(v):
    return (v, None)

def back_low(kept, grad):
    return (low(grad),)
low.defvjp(low_keep, low_pass)
low_back.defvjp(back_keep, back_low)
NORM_EPSILON = 1e-05
MASKED_SCORE = -1e+30

def both_ways(inputs):
    return low_back(low(inputs))

def matmul(left, right):
    return jnp.dot(left, right, precision=lax.Precision.HIGHEST, preferred_element_type=jnp.float32)

def normalize(inputs, gain_row, shift_row):
    center = lax.optimization_barrier(jnp.mean(inputs, -1, keepdims=True))
    centered = inputs - center
    variance = lax.optimization_barrier(jnp.mean(centered * centered, -1, keepdims=True))
    return centered * lax.rsqrt(variance + NORM_EPSILON) * gain_row + shift_row

def attend_slot(element):
    query_rows, key_rows, value_rows, length_now = element
    slot_rows = query_rows.shape[0]
    score_scale = 1.0 / math.sqrt(HEAD_DIM)
    query_heads = query_rows.reshape(slot_rows, HEADS, HEAD_DIM)
    key_heads = key_rows.reshape(slot_rows, HEADS, HEAD_DIM)
    value_heads = value_rows.reshape(slot_rows, HEADS, HEAD_DIM)
    scores = jnp.einsum('qhd,khd->hqk', query_heads, key_heads, precision=lax.Precision.HIGHEST) * score_scale
    scores = low_back(scores)
    places = jnp.arange(slot_rows, dtype=jnp.int32)
    allowed = (places[None, :] <= places[:, None]) & (places[None, :] < length_now)
    scores = jnp.where(allowed[None], scores, MASKED_SCORE)
    maximum = lax.optimization_barrier(jnp.max(scores, -1, keepdims=True))
    raised = jnp.exp(scores - maximum)
    softmax_w = low(raised / lax.optimization_barrier(jnp.sum(raised, -1, keepdims=True)))
    attended = jnp.einsum('hqk,khd->qhd', softmax_w, value_heads, precision=lax.Precision.HIGHEST)
    return attended.reshape(slot_rows, D)

def block_forward(inputs, gains, biases, w_in, w_out, w_expand, w_project, tie_map, live_mask, slot_lengths):
    gain_one = gains[tie_map[0], 0]
    gain_two = gains[tie_map[2], 1]
    shift_one = biases[tie_map[0], 0]
    query_bias = biases[tie_map[0], 1]
    value_bias = biases[tie_map[0], 2]
    out_bias = biases[tie_map[1], 3]
    shift_two = biases[tie_map[2], 4]
    project_bias = biases[tie_map[3], 5]
    expand_bias = biases[tie_map[2], 6:].reshape(FF)
    in_mats = w_in[tie_map[0]]
    out_mat = w_out[tie_map[1]]
    expand_mat = w_expand[tie_map[2]]
    project_mat = w_project[tie_map[3]]
    local_width = D // N_TENSOR
    hidden_width = FF // N_TENSOR
    normed_one = normalize(inputs, gain_one, shift_one)
    queries, key_parts, value_parts = ([], [], [])
    for group_index in range(N_TENSOR):
        columns = slice(group_index * local_width, (group_index + 1) * local_width)
        shared = both_ways(normed_one)
        queries.append(both_ways(matmul(shared, in_mats[0][:, columns]) + query_bias[columns]))
        key_parts.append(both_ways(matmul(shared, in_mats[1][:, columns])))
        value_parts.append(both_ways(matmul(shared, in_mats[2][:, columns]) + value_bias[columns]))
    slot_count = slot_lengths.shape[0]
    query_all = jnp.concatenate(queries, 1).reshape(slot_count, SLOT_LEN, D)
    key_all = jnp.concatenate(key_parts, 1).reshape(slot_count, SLOT_LEN, D)
    value_all = jnp.concatenate(value_parts, 1).reshape(slot_count, SLOT_LEN, D)
    attended = lax.map(jax.checkpoint(attend_slot), (query_all, key_all, value_all, slot_lengths))
    attended = both_ways(attended.reshape(slot_count * SLOT_LEN, D))
    branch_sum = None
    for group_index in range(N_TENSOR):
        columns = slice(group_index * local_width, (group_index + 1) * local_width)
        term = low(matmul(attended[:, columns], out_mat[columns, :]))
        branch_sum = term if branch_sum is None else branch_sum + term
    branch = low_back(branch_sum + out_bias)
    residual = inputs + branch
    normed_two = normalize(residual, gain_two, shift_two)
    feed_sum = None
    for group_index in range(N_TENSOR):
        hidden_cols = slice(group_index * hidden_width, (group_index + 1) * hidden_width)
        shared = both_ways(normed_two)
        expanded = low_back(matmul(shared, expand_mat[:, hidden_cols]) + expand_bias[hidden_cols])
        activated = low(jax.nn.gelu(expanded, approximate=True))
        term = low(matmul(activated, project_mat[hidden_cols, :]))
        feed_sum = term if feed_sum is None else feed_sum + term
    feed = low_back(feed_sum + project_bias)
    return live_mask * (residual + feed)

def reference(tokens, lengths, tie_map, norm_gains, bias_rows, attention_in, attention_out, expand_weight, project_weight, cotangent):
    weights = (norm_gains.astype(jnp.float32), bias_rows.astype(jnp.float32), attention_in.astype(jnp.float32), attention_out.astype(jnp.float32), expand_weight.astype(jnp.float32), project_weight.astype(jnp.float32))
    block_rows = SLOT_DEV * SLOT_LEN
    inputs_all = tokens.astype(jnp.float32).reshape(N_DP, block_rows, D)
    cot_all = cotangent.astype(jnp.float32).reshape(N_DP, block_rows, D)
    length_all = lengths.reshape(N_DP, SLOT_DEV)

    def scan_step(totals, element):
        block_in, block_cot, block_len = element
        places = jnp.arange(SLOT_LEN, dtype=jnp.int32)
        live_mask = (places[None, :] < block_len[:, None]).reshape(block_rows, 1).astype(jnp.float32)

        def apply_block(block_inputs, *params):
            return block_forward(block_inputs, *params, tie_map, live_mask, block_len)
        outputs, pullback = jax.vjp(apply_block, block_in, *weights)
        gradients = pullback(block_cot)
        totals = tuple((acc + new for acc, new in zip(totals, gradients[1:])))
        return (totals, (outputs.astype(jnp.bfloat16), gradients[0].astype(jnp.bfloat16)))
    initial = tuple((jnp.zeros_like(item_w) for item_w in weights))
    totals, (outputs, input_grads) = lax.scan(scan_step, initial, (inputs_all, cot_all, length_all))
    return (outputs.reshape(TOKENS, D), input_grads.reshape(TOKENS, D), totals[0], totals[1], totals[2], totals[3], totals[4], totals[5])
```

```python
from functools import partial

import jax
import jax.numpy as jnp
from jax import lax
from jax.experimental import pallas as pl
from jax.experimental.pallas import tpu as pltpu
from jax.sharding import PartitionSpec as P

D = 768
HEAD_DIM = 64
FF = 3072
NSRC = 4
EPS = 1e-05
MASKED = -1e30
F32 = jnp.float32
BF16 = jnp.bfloat16
VMEM_LIMIT = 60 * 1024 * 1024


def dot_nn(a, b):
    return lax.dot_general(a, b, (((1,), (0,)), ((), ())), preferred_element_type=F32)


def dot_nt(a, b):
    return lax.dot_general(a, b, (((1,), (1,)), ((), ())), preferred_element_type=F32)


def norm_parts(v):
    center = jnp.mean(v, -1, keepdims=True)
    centered = v - center
    r = lax.rsqrt(jnp.mean(centered * centered, -1, keepdims=True) + EPS)
    return centered * r, r


def head_mask(shape, h):
    lane = lax.broadcasted_iota(jnp.int32, shape, 1)
    return (lane >= h * HEAD_DIM) & (lane < (h + 1) * HEAD_DIM)


def blocks(total, size):
    return [slice(i * size, (i + 1) * size) for i in range(total // size)]


def attention_forward(
    len_ref, x_ref, g_ref, rows_ref, bqv_ref,
    q_ref, v_ref, kt_ref, p_ref, o_ref, a1t_ref, h1_ref, a2_ref, a2t_ref,
    a1_ref, k_ref, vt_ref, ot_ref, attn_ref,
):
    t = pl.program_id(0)
    n = x_ref.shape[0]
    width = g_ref.shape[-1]
    heads = width // HEAD_DIM
    step = 256
    length = len_ref[0]

    @pl.when(t == 0)
    def _():
        @pl.loop(0, n // step)
        def _(b):
            rows = pl.ds(pl.multiple_of(b * step, step), step)
            xhat, _ = norm_parts(x_ref[rows, :].astype(F32))
            a1 = xhat * rows_ref[0:1, :] + rows_ref[2:3, :]
            a1_ref[rows, :] = a1.astype(BF16)
            a1t_ref[:, rows] = a1.astype(BF16).T
            attn_ref[rows, :] = x_ref[rows, :].astype(F32) + rows_ref[5:6, :]

    @pl.loop(0, n // step)
    def _(b):
        rows = pl.ds(pl.multiple_of(b * step, step), step)
        a1 = a1_ref[rows, :]
        q = (dot_nn(a1, g_ref[0, 0]) + bqv_ref[0, 0:1, :]).astype(BF16)
        q_ref[0, rows, :] = q * jnp.asarray(HEAD_DIM ** -0.5, BF16)
        k = dot_nn(a1, g_ref[0, 1]).astype(BF16)
        k_ref[rows, :] = k
        kt_ref[0, :, rows] = k.T
        v = (dot_nn(a1, g_ref[0, 2]) + bqv_ref[0, 1:2, :]).astype(BF16)
        v_ref[0, rows, :] = v
        vt_ref[:, rows] = v.T

    for h in range(heads):
        k = k_ref[...]
        k = jnp.where(head_mask(k.shape, h), k, jnp.zeros_like(k))
        for b in range(n // step):
            first, last = b * step, (b + 1) * step
            q = q_ref[0, first:last, :]
            key = lax.broadcasted_iota(jnp.int32, (last, step), 0)
            query = lax.broadcasted_iota(jnp.int32, (step, step), 1) + first
            s = dot_nt(k[:last], q)
            near = jnp.where(
                (key[first:] <= query) & (key[first:] < length), s[first:], MASKED
            )
            if b:
                far = jnp.where(key[:first] < length, s[:first], MASKED)
                top = jnp.maximum(
                    jnp.max(far, 0, keepdims=True), jnp.max(near, 0, keepdims=True)
                )
                e_far = jnp.exp(far - top)
                e_near = jnp.exp(near - top)
                total = jnp.sum(e_far, 0, keepdims=True) + jnp.sum(e_near, 0, keepdims=True)
                scale = 1.0 / total
                p_ref[0, h, :first, first:last] = (e_far * scale).astype(BF16)
            else:
                top = jnp.max(near, 0, keepdims=True)
                e_near = jnp.exp(near - top)
                scale = 1.0 / jnp.sum(e_near, 0, keepdims=True)
            p_ref[0, h, first:last, first:last] = (e_near * scale).astype(BF16)
            ot_ref[h * HEAD_DIM : (h + 1) * HEAD_DIM, first:last] = dot_nn(
                vt_ref[h * HEAD_DIM : (h + 1) * HEAD_DIM, :last],
                p_ref[0, h, :last, first:last],
            ).astype(BF16)

    @pl.loop(0, n // step)
    def _(b):
        rows = pl.ds(pl.multiple_of(b * step, step), step)
        o = ot_ref[:, rows].T
        o_ref[0, rows, :] = o
        attn_ref[rows, :] += dot_nt(o, g_ref[0, 3])

    @pl.when(t == pl.num_programs(0) - 1)
    def _():
        @pl.loop(0, n // step)
        def _(b):
            rows = pl.ds(pl.multiple_of(b * step, step), step)
            h1 = attn_ref[rows, :]
            h1_ref[rows, :] = h1
            xhat, _ = norm_parts(h1)
            a2 = (xhat * rows_ref[1:2, :] + rows_ref[6:7, :]).astype(BF16)
            a2_ref[rows, :] = a2
            a2t_ref[:, rows] = a2.T


SQRT_2_PI = 0.7978845608028654


def feed_forward_both(
    len_ref, c_ref, a2_ref, a2t_ref, h1_ref, w1_ref, w2_ref, rows_ref,
    out_ref, d1_ref, d2_ref, dh1_ref, gb_ref, gbt_ref, sums_ref,
    gf_ref, gft_ref, feed_ref, da2_ref, h_ref, df_ref,
):
    t = pl.program_id(0)
    n = c_ref.shape[0]
    step = 256
    length = len_ref[0]

    @pl.when(t == 0)
    def _():
        sums_ref[...] = jnp.zeros_like(sums_ref)

        @pl.loop(0, n // step)
        def _(b):
            rows = pl.ds(pl.multiple_of(b * step, step), step)
            place = b * step + lax.broadcasted_iota(jnp.int32, (step, 1), 0)
            live = (place < length).astype(F32)
            g = (c_ref[rows, :].astype(F32) * live).astype(BF16)
            gf_ref[rows, :] = g
            gft_ref[:, rows] = g.T
            sums_ref[7:8, :] += jnp.sum(g.astype(F32), 0, keepdims=True)

    bias = rows_ref[pl.ds(8 + t, 1), :]

    @pl.loop(0, n // step)
    def _(b):
        rows = pl.ds(pl.multiple_of(b * step, step), step)
        f = dot_nn(a2_ref[rows, :], w1_ref[0]) + bias
        dh = dot_nn(gf_ref[rows, :], w2_ref[0])
        f2 = f * f
        th = jnp.tanh(f * (SQRT_2_PI + (SQRT_2_PI * 0.044715) * f2))
        half = 0.5 + 0.5 * th
        h = (f * half).astype(BF16)
        slope = half + f * (0.5 - 0.5 * th * th) * (
            SQRT_2_PI + (3 * SQRT_2_PI * 0.044715) * f2
        )
        df = (dh * slope).astype(BF16)
        h_ref[rows, :] = h
        df_ref[rows, :] = df
        sums_ref[pl.ds(8 + t, 1), :] += jnp.sum(df.astype(F32), 0, keepdims=True)
        feed = dot_nt(h, w2_ref[0])
        da2 = dot_nt(df, w1_ref[0])

        @pl.when(t == 0)
        def _():
            feed_ref[rows, :] = feed
            da2_ref[rows, :] = da2

        @pl.when(t > 0)
        def _():
            feed_ref[rows, :] += feed
            da2_ref[rows, :] += da2

    @pl.loop(0, D // step)
    def _(b):
        rows = pl.ds(pl.multiple_of(b * step, step), step)
        d1_ref[0, rows, :] = dot_nn(a2t_ref[rows, :], df_ref[...]).astype(BF16)
        d2_ref[0, rows, :] = dot_nn(gft_ref[rows, :], h_ref[...]).astype(BF16)

    @pl.when(t == pl.num_programs(0) - 1)
    def _():
        @pl.loop(0, n // step)
        def _(b):
            rows = pl.ds(pl.multiple_of(b * step, step), step)
            place = b * step + lax.broadcasted_iota(jnp.int32, (step, 1), 0)
            live = (place < length).astype(F32)
            h1 = h1_ref[rows, :]
            out_ref[rows, :] = (live * (h1 + (feed_ref[rows, :] + rows_ref[7:8, :]))).astype(BF16)
            xhat, r = norm_parts(h1)
            da2 = da2_ref[rows, :]
            sums_ref[1:2, :] += jnp.sum(da2 * xhat, 0, keepdims=True)
            sums_ref[6:7, :] += jnp.sum(da2, 0, keepdims=True)
            dg = da2 * rows_ref[1:2, :]
            dv = r * (
                dg
                - jnp.mean(dg, -1, keepdims=True)
                - xhat * jnp.mean(dg * xhat, -1, keepdims=True)
            )
            dh1 = live * c_ref[rows, :].astype(F32) + dv
            dh1_ref[rows, :] = dh1
            gb = dh1.astype(BF16)
            gb_ref[rows, :] = gb
            gbt_ref[:, rows] = gb.T
            sums_ref[5:6, :] += jnp.sum(gb.astype(F32), 0, keepdims=True)


def attention_backward(
    x_ref, g_ref, rows_ref, dh1_ref, gb_ref, gbt_ref, q_ref, v_ref, kt_ref, p_ref,
    o_ref, a1t_ref,
    d0_ref, xg_ref, sums_ref, bqv_ref,
    do_ref, delta_ref, dqt_ref, dq_ref, dk_ref, dv_ref, da1_ref,
):
    t = pl.program_id(0)
    n = x_ref.shape[0]
    width = g_ref.shape[-1]
    heads = width // HEAD_DIM
    step = 256
    pick = (
        lax.broadcasted_iota(jnp.int32, (16, width), 1) // HEAD_DIM
        == lax.broadcasted_iota(jnp.int32, (16, width), 0)
    ).astype(BF16)

    @pl.loop(0, n // step)
    def _(b):
        rows = pl.ds(pl.multiple_of(b * step, step), step)
        do = dot_nn(gb_ref[rows, :], g_ref[0, 3]).astype(BF16)
        do_ref[rows, :] = do
        prod = do.astype(F32) * o_ref[0, rows, :].astype(F32)
        high = prod.astype(BF16)
        low = (prod - high.astype(F32)).astype(BF16)
        delta_ref[:, rows] = dot_nt(pick, high) + dot_nt(pick, low)

    dqt_ref[...] = jnp.zeros_like(dqt_ref)
    for b in range(n // step):
        first, last = b * step, (b + 1) * step
        do = do_ref[first:, :]
        q = q_ref[0, first:, :]
        v = v_ref[0, first:last, :]
        dk, dv = None, None
        for h in range(heads):
            mine = head_mask((1, width), h)
            zero = jnp.zeros((), BF16)
            p = p_ref[0, h, first:last, first:]
            dp = dot_nt(jnp.where(mine, v, zero), do)
            ds = (p.astype(F32) * (dp - delta_ref[h : h + 1, first:])).astype(BF16)
            part = dot_nn(p, jnp.where(mine, do, zero))
            dv = part if dv is None else dv + part
            part = dot_nn(ds, jnp.where(mine, q, zero))
            dk = part if dk is None else dk + part
            head = slice(h * HEAD_DIM, (h + 1) * HEAD_DIM)
            dqt_ref[head, first:] += dot_nn(kt_ref[0, head, first:last], ds)
        dk_ref[first:last, :] = dk.astype(BF16)
        dv_ref[first:last, :] = dv.astype(BF16)

    @pl.when(t == 0)
    def _():
        da1_ref[...] = jnp.zeros_like(da1_ref)

    bqv_ref[...] = jnp.zeros_like(bqv_ref)

    @pl.loop(0, n // step)
    def _(b):
        rows = pl.ds(pl.multiple_of(b * step, step), step)
        dq = (dqt_ref[:, rows] * HEAD_DIM ** -0.5).astype(BF16).T
        dk = dk_ref[rows, :]
        dv = dv_ref[rows, :]
        dq_ref[rows, :] = dq
        bqv_ref[0, 0:1, :] += jnp.sum(dq.astype(F32), 0, keepdims=True)
        bqv_ref[0, 1:2, :] += jnp.sum(dv.astype(F32), 0, keepdims=True)
        da1_ref[rows, :] += (
            dot_nt(dq, g_ref[0, 0]) + dot_nt(dk, g_ref[0, 1]) + dot_nt(dv, g_ref[0, 2])
        )

    @pl.loop(0, D // step)
    def _(b):
        rows = pl.ds(pl.multiple_of(b * step, step), step)
        a1t = a1t_ref[rows, :]
        d0_ref[0, 0, rows, :] = dot_nn(a1t, dq_ref[...]).astype(BF16)
        d0_ref[0, 1, rows, :] = dot_nn(a1t, dk_ref[...]).astype(BF16)
        d0_ref[0, 2, rows, :] = dot_nn(a1t, dv_ref[...]).astype(BF16)
        d0_ref[0, 3, rows, :] = dot_nn(gbt_ref[rows, :], o_ref[0]).astype(BF16)

    @pl.when(t == pl.num_programs(0) - 1)
    def _():
        sums_ref[...] = jnp.zeros_like(sums_ref)

        @pl.loop(0, n // step)
        def _(b):
            rows = pl.ds(pl.multiple_of(b * step, step), step)
            xhat, r = norm_parts(x_ref[rows, :].astype(F32))
            da1 = da1_ref[rows, :]
            sums_ref[0:1, :] += jnp.sum(da1 * xhat, 0, keepdims=True)
            sums_ref[1:2, :] += jnp.sum(da1, 0, keepdims=True)
            dg = da1 * rows_ref[0:1, :]
            dv = r * (
                dg
                - jnp.mean(dg, -1, keepdims=True)
                - xhat * jnp.mean(dg * xhat, -1, keepdims=True)
            )
            xg_ref[rows, :] = (dh1_ref[rows, :] + dv).astype(BF16)


def whole(*shape):
    return pl.BlockSpec(shape, lambda t: (0,) * len(shape))


def group(*shape):
    return pl.BlockSpec((1,) + shape, lambda t: (t,) + (0,) * len(shape))


def shaped(dtype, *shape):
    return jax.ShapeDtypeStruct(shape, dtype)


SMEM_WHOLE = pl.BlockSpec(memory_space=pltpu.SMEM)


def run_attention_forward(length, x, g0, rows, bqv):
    n = x.shape[0]
    groups, _, _, width = g0.shape
    heads = width // HEAD_DIM
    return pl.pallas_call(
        attention_forward,
        grid=(groups,),
        in_specs=[SMEM_WHOLE, whole(n, D), group(4, D, width), whole(16, D), group(2, width)],
        out_specs=[
            group(n, width), group(n, width), group(width, n), group(heads, n, n),
            group(n, width), whole(D, n), whole(n, D), whole(n, D), whole(D, n),
        ],
        out_shape=[
            shaped(BF16, groups, n, width), shaped(BF16, groups, n, width),
            shaped(BF16, groups, width, n), shaped(BF16, groups, heads, n, n),
            shaped(BF16, groups, n, width), shaped(BF16, D, n), shaped(F32, n, D),
            shaped(BF16, n, D), shaped(BF16, D, n),
        ],
        scratch_shapes=[
            pltpu.VMEM((n, D), BF16), pltpu.VMEM((n, width), BF16),
            pltpu.VMEM((width, n), BF16), pltpu.VMEM((width, n), BF16),
            pltpu.VMEM((n, D), F32),
        ],
        compiler_params=pltpu.CompilerParams(vmem_limit_bytes=VMEM_LIMIT),
        name="attention_forward",
    )(length, x, g0, rows, bqv)


def run_feed_forward(length, cot, a2, a2t, h1, g1, g2, rows):
    n = cot.shape[0]
    groups, _, width = g1.shape
    return pl.pallas_call(
        feed_forward_both,
        grid=(groups,),
        in_specs=[
            SMEM_WHOLE, whole(n, D), whole(n, D), whole(D, n), whole(n, D),
            group(D, width), group(D, width), whole(16, D),
        ],
        out_specs=[
            whole(n, D), group(D, width), group(D, width), whole(n, D), whole(n, D),
            whole(D, n), whole(16, D),
        ],
        out_shape=[
            shaped(BF16, n, D), shaped(BF16, groups, D, width), shaped(BF16, groups, D, width),
            shaped(F32, n, D), shaped(BF16, n, D), shaped(BF16, D, n), shaped(F32, 16, D),
        ],
        scratch_shapes=[
            pltpu.VMEM((n, D), BF16), pltpu.VMEM((D, n), BF16), pltpu.VMEM((n, D), F32),
            pltpu.VMEM((n, D), F32), pltpu.VMEM((n, width), BF16), pltpu.VMEM((n, width), BF16),
        ],
        compiler_params=pltpu.CompilerParams(vmem_limit_bytes=VMEM_LIMIT),
        name="feed_forward_both",
    )(length, cot, a2, a2t, h1, g1, g2, rows)


def run_attention_backward(x, g0, rows, dh1, gb, gbt, q, v, kt, p, o, a1t):
    n = x.shape[0]
    groups, _, _, width = g0.shape
    heads = width // HEAD_DIM
    return pl.pallas_call(
        attention_backward,
        grid=(groups,),
        in_specs=[
            whole(n, D), group(4, D, width), whole(16, D), whole(n, D), whole(n, D),
            whole(D, n), group(n, width), group(n, width), group(width, n),
            group(heads, n, n), group(n, width), whole(D, n),
        ],
        out_specs=[group(4, D, width), whole(n, D), whole(8, D), group(8, width)],
        out_shape=[
            shaped(BF16, groups, 4, D, width), shaped(BF16, n, D), shaped(F32, 8, D),
            shaped(F32, groups, 8, width),
        ],
        scratch_shapes=[
            pltpu.VMEM((n, width), BF16), pltpu.VMEM((16, n), F32), pltpu.VMEM((width, n), F32),
            pltpu.VMEM((n, width), BF16), pltpu.VMEM((n, width), BF16),
            pltpu.VMEM((n, width), BF16), pltpu.VMEM((n, D), F32),
        ],
        compiler_params=pltpu.CompilerParams(vmem_limit_bytes=VMEM_LIMIT),
        name="attention_backward",
    )(x, g0, rows, dh1, gb, gbt, q, v, kt, p, o, a1t)


def on_device(
    tokens, lengths, tie_map, norm_gains, bias_rows, attention_in, attention_out,
    expand_weight, project_weight, cotangent,
):
    both = ("dp", "tensor")
    slot_rows = tokens.shape[0] // lengths.shape[0]
    me = lax.axis_index("tensor")
    in_local = lax.dynamic_index_in_dim(attention_in, tie_map[0], 0, keepdims=False)
    out_local = lax.dynamic_index_in_dim(attention_out, tie_map[1], 0, keepdims=False)
    expand_local = lax.dynamic_index_in_dim(expand_weight, tie_map[2], 0, keepdims=False)
    project_local = lax.dynamic_index_in_dim(project_weight, tie_map[3], 0, keepdims=False)
    local0 = jnp.concatenate([in_local, out_local.T[None]], 0)
    row_kinds = jnp.array([0, 0, 0, 1, 2, 3] + [2] * (FF // D), dtype=jnp.int32)
    gain_kinds = jnp.array([0, 2], dtype=jnp.int32)
    gain_pick = norm_gains[tie_map[gain_kinds], jnp.arange(2)]
    bias_pick = bias_rows[tie_map[row_kinds], jnp.arange(row_kinds.shape[0])]
    vectors = jnp.concatenate([gain_pick, bias_pick], 0)
    rows = lax.all_gather(vectors, both, axis=1, tiled=True).astype(F32)
    rows = jnp.concatenate([rows, jnp.zeros((4, D), F32)], 0)

    def gathered(piece, axis):
        piece = lax.all_gather(piece, "dp", axis=axis, tiled=True)
        return lax.all_gather(piece, "tensor", axis=0)

    g0 = gathered(local0, 1)
    g1 = gathered(expand_local, 0)
    g2 = gathered(project_local.T, 0)
    groups, width = g0.shape[0], g0.shape[-1]
    bqv = rows[3:5].reshape(2, groups, width).transpose(1, 0, 2)

    x = lax.dynamic_slice_in_dim(tokens, me * slot_rows, slot_rows, 0)
    cot = lax.dynamic_slice_in_dim(cotangent, me * slot_rows, slot_rows, 0)
    length = lax.dynamic_slice_in_dim(lengths, me, 1, 0)

    q, v, kt, p, o, a1t, h1, a2, a2t = run_attention_forward(length, x, g0, rows, bqv)
    out, d1, d2, dh1, gb, gbt, sums = run_feed_forward(length, cot, a2, a2t, h1, g1, g2, rows)
    d0, xg, sums_in, sums_qv = run_attention_backward(
        x, g0, rows, dh1, gb, gbt, q, v, kt, p, o, a1t
    )
    layer_out = lax.all_gather(out, "tensor", axis=0, tiled=True)
    tokens_grad = lax.all_gather(xg, "tensor", axis=0, tiled=True)

    def scattered(piece, axis):
        piece = lax.psum_scatter(piece, "tensor", scatter_dimension=0)
        return lax.psum_scatter(piece, "dp", scatter_dimension=axis, tiled=True).astype(F32)

    part0 = scattered(d0, 1)
    part1 = scattered(d1, 0)
    part2 = scattered(d2, 0)
    qv = sums_qv[:, :2].transpose(1, 0, 2).reshape(2, D)
    sums = jnp.concatenate(
        [sums_in[0:1], sums[1:2], sums_in[1:2], qv, sums[5:12]], 0
    )
    sums = lax.psum_scatter(sums, both, scatter_dimension=1, tiled=True)
    return layer_out, tokens_grad, *placed(tie_map, sums, part0, part1, part2)


def placed(tie_map, sums, part0, part1, part2):
    source = jnp.arange(NSRC, dtype=jnp.int32)

    def place(piece, which):
        pick = (source == tie_map[which]).reshape((NSRC,) + (1,) * piece.ndim)
        return jnp.where(pick, piece[None], 0.0)

    def place_rows(piece, kinds):
        pick = source[:, None] == tie_map[jnp.array(kinds, dtype=jnp.int32)][None, :]
        return jnp.where(pick[:, :, None], piece[None], 0.0)

    return (
        place_rows(sums[:2], [0, 2]),
        place_rows(sums[2:], [0, 0, 0, 1, 2, 3] + [2] * (FF // D)),
        place(part0[:3], 0),
        place(part0[3].T, 1),
        place(part1, 2),
        place(part2.T, 3),
    )


def solution(mesh):
    return jax.shard_map(
        on_device,
        mesh=mesh,
        in_specs=(
            P("dp", None),
            P("dp"),
            P(),
            P(None, None, ("dp", "tensor")),
            P(None, None, ("dp", "tensor")),
            P(None, None, "dp", "tensor"),
            P(None, "tensor", "dp"),
            P(None, "dp", "tensor"),
            P(None, "tensor", "dp"),
            P("dp", None),
        ),
        out_specs=(
            P("dp", None),
            P("dp", None),
            P(None, None, ("dp", "tensor")),
            P(None, None, ("dp", "tensor")),
            P(None, None, "dp", "tensor"),
            P(None, "tensor", "dp"),
            P(None, "dp", "tensor"),
            P(None, "tensor", "dp"),
        ),
        check_vma=False,
    )
```

```python
from functools import partial

import jax
import jax.numpy as jnp
from jax import lax
from jax.experimental import pallas as pl
from jax.experimental.pallas import tpu as pltpu
from jax.sharding import PartitionSpec as P

D = 768
HEAD_DIM = 64
FF = 3072
NSRC = 4
EPS = 1e-05
MASKED = -1e30
F32 = jnp.float32
BF16 = jnp.bfloat16
VMEM_LIMIT = 60 * 1024 * 1024


def dot_nn(a, b):
    return lax.dot_general(a, b, (((1,), (0,)), ((), ())), preferred_element_type=F32)


def dot_nt(a, b):
    return lax.dot_general(a, b, (((1,), (1,)), ((), ())), preferred_element_type=F32)


def norm_parts(v):
    center = jnp.mean(v, -1, keepdims=True)
    centered = v - center
    r = lax.rsqrt(jnp.mean(centered * centered, -1, keepdims=True) + EPS)
    return centered * r, r


def head_mask(shape, h):
    lane = lax.broadcasted_iota(jnp.int32, shape, 1)
    return (lane >= h * HEAD_DIM) & (lane < (h + 1) * HEAD_DIM)


def blocks(total, size):
    return [slice(i * size, (i + 1) * size) for i in range(total // size)]


def attention_forward(
    len_ref, x_ref, g_ref, rows_ref, bqv_ref,
    q_ref, v_ref, kt_ref, p_ref, o_ref, a1t_ref, h1_ref, a2_ref, a2t_ref,
    a1_ref, k_ref, vt_ref, ot_ref, attn_ref,
):
    t = pl.program_id(0)
    n = x_ref.shape[0]
    width = g_ref.shape[-1]
    heads = width // HEAD_DIM
    step = 256
    length = len_ref[0]

    @pl.when(t == 0)
    def _():
        @pl.loop(0, n // step)
        def _(b):
            rows = pl.ds(pl.multiple_of(b * step, step), step)
            xhat, _ = norm_parts(x_ref[rows, :].astype(F32))
            a1 = xhat * rows_ref[0:1, :] + rows_ref[2:3, :]
            a1_ref[rows, :] = a1.astype(BF16)
            a1t_ref[:, rows] = a1.astype(BF16).T
            attn_ref[rows, :] = x_ref[rows, :].astype(F32) + rows_ref[5:6, :]

    @pl.loop(0, n // step)
    def _(b):
        rows = pl.ds(pl.multiple_of(b * step, step), step)
        a1 = a1_ref[rows, :]
        q = (dot_nn(a1, g_ref[0, 0]) + bqv_ref[0, 0:1, :]).astype(BF16)
        q_ref[0, rows, :] = q * jnp.asarray(HEAD_DIM ** -0.5, BF16)
        k = dot_nn(a1, g_ref[0, 1]).astype(BF16)
        k_ref[rows, :] = k
        kt_ref[0, :, rows] = k.T
        v = (dot_nn(a1, g_ref[0, 2]) + bqv_ref[0, 1:2, :]).astype(BF16)
        v_ref[0, rows, :] = v
        vt_ref[:, rows] = v.T

    for h in range(heads):
        k = k_ref[...]
        k = jnp.where(head_mask(k.shape, h), k, jnp.zeros_like(k))
        for b in range(n // step):
            first, last = b * step, (b + 1) * step
            q = q_ref[0, first:last, :]
            key = lax.broadcasted_iota(jnp.int32, (last, step), 0)
            query = lax.broadcasted_iota(jnp.int32, (step, step), 1) + first
            s = dot_nt(k[:last], q)
            near = jnp.where(
                (key[first:] <= query) & (key[first:] < length), s[first:], MASKED
            )
            if b:
                far = jnp.where(key[:first] < length, s[:first], MASKED)
                top = jnp.maximum(
                    jnp.max(far, 0, keepdims=True), jnp.max(near, 0, keepdims=True)
                )
                e_far = jnp.exp(far - top)
                e_near = jnp.exp(near - top)
                total = jnp.sum(e_far, 0, keepdims=True) + jnp.sum(e_near, 0, keepdims=True)
                scale = 1.0 / total
                p_ref[0, h, :first, first:last] = (e_far * scale).astype(BF16)
            else:
                top = jnp.max(near, 0, keepdims=True)
                e_near = jnp.exp(near - top)
                scale = 1.0 / jnp.sum(e_near, 0, keepdims=True)
            p_ref[0, h, first:last, first:last] = (e_near * scale).astype(BF16)
            ot_ref[h * HEAD_DIM : (h + 1) * HEAD_DIM, first:last] = dot_nn(
                vt_ref[h * HEAD_DIM : (h + 1) * HEAD_DIM, :last],
                p_ref[0, h, :last, first:last],
            ).astype(BF16)

    @pl.loop(0, n // step)
    def _(b):
        rows = pl.ds(pl.multiple_of(b * step, step), step)
        o = ot_ref[:, rows].T
        o_ref[0, rows, :] = o
        attn_ref[rows, :] += dot_nt(o, g_ref[0, 3])

    @pl.when(t == pl.num_programs(0) - 1)
    def _():
        @pl.loop(0, n // step)
        def _(b):
            rows = pl.ds(pl.multiple_of(b * step, step), step)
            h1 = attn_ref[rows, :]
            h1_ref[rows, :] = h1
            xhat, _ = norm_parts(h1)
            a2 = (xhat * rows_ref[1:2, :] + rows_ref[6:7, :]).astype(BF16)
            a2_ref[rows, :] = a2
            a2t_ref[:, rows] = a2.T


SQRT_2_PI = 0.7978845608028654


def feed_forward_both(
    len_ref, c_ref, a2_ref, a2t_ref, h1_ref, w1_ref, w2_ref, rows_ref,
    out_ref, d1_ref, d2_ref, dh1_ref, gb_ref, gbt_ref, sums_ref,
    gf_ref, gft_ref, feed_ref, da2_ref, h_ref, df_ref,
):
    t = pl.program_id(0)
    n = c_ref.shape[0]
    step = 256
    length = len_ref[0]

    @pl.when(t == 0)
    def _():
        sums_ref[...] = jnp.zeros_like(sums_ref)

        @pl.loop(0, n // step)
        def _(b):
            rows = pl.ds(pl.multiple_of(b * step, step), step)
            place = b * step + lax.broadcasted_iota(jnp.int32, (step, 1), 0)
            live = (place < length).astype(F32)
            g = (c_ref[rows, :].astype(F32) * live).astype(BF16)
            gf_ref[rows, :] = g
            gft_ref[:, rows] = g.T
            sums_ref[7:8, :] += jnp.sum(g.astype(F32), 0, keepdims=True)

    bias = rows_ref[pl.ds(8 + t, 1), :]

    @pl.loop(0, n // step)
    def _(b):
        rows = pl.ds(pl.multiple_of(b * step, step), step)
        f = dot_nn(a2_ref[rows, :], w1_ref[0]) + bias
        dh = dot_nn(gf_ref[rows, :], w2_ref[0])
        f2 = f * f
        th = jnp.tanh(f * (SQRT_2_PI + (SQRT_2_PI * 0.044715) * f2))
        half = 0.5 + 0.5 * th
        h = (f * half).astype(BF16)
        slope = half + f * (0.5 - 0.5 * th * th) * (
            SQRT_2_PI + (3 * SQRT_2_PI * 0.044715) * f2
        )
        df = (dh * slope).astype(BF16)
        h_ref[rows, :] = h
        df_ref[rows, :] = df
        sums_ref[pl.ds(8 + t, 1), :] += jnp.sum(df.astype(F32), 0, keepdims=True)
        feed = dot_nt(h, w2_ref[0])
        da2 = dot_nt(df, w1_ref[0])

        @pl.when(t == 0)
        def _():
            feed_ref[rows, :] = feed
            da2_ref[rows, :] = da2

        @pl.when(t > 0)
        def _():
            feed_ref[rows, :] += feed
            da2_ref[rows, :] += da2

    @pl.loop(0, D // step)
    def _(b):
        rows = pl.ds(pl.multiple_of(b * step, step), step)
        d1_ref[0, rows, :] = dot_nn(a2t_ref[rows, :], df_ref[...]).astype(BF16)
        d2_ref[0, rows, :] = dot_nn(gft_ref[rows, :], h_ref[...]).astype(BF16)

    @pl.when(t == pl.num_programs(0) - 1)
    def _():
        @pl.loop(0, n // step)
        def _(b):
            rows = pl.ds(pl.multiple_of(b * step, step), step)
            place = b * step + lax.broadcasted_iota(jnp.int32, (step, 1), 0)
            live = (place < length).astype(F32)
            h1 = h1_ref[rows, :]
            out_ref[rows, :] = (live * (h1 + (feed_ref[rows, :] + rows_ref[7:8, :]))).astype(BF16)
            xhat, r = norm_parts(h1)
            da2 = da2_ref[rows, :]
            sums_ref[1:2, :] += jnp.sum(da2 * xhat, 0, keepdims=True)
            sums_ref[6:7, :] += jnp.sum(da2, 0, keepdims=True)
            dg = da2 * rows_ref[1:2, :]
            dv = r * (
                dg
                - jnp.mean(dg, -1, keepdims=True)
                - xhat * jnp.mean(dg * xhat, -1, keepdims=True)
            )
            dh1 = live * c_ref[rows, :].astype(F32) + dv
            dh1_ref[rows, :] = dh1
            gb = dh1.astype(BF16)
            gb_ref[rows, :] = gb
            gbt_ref[:, rows] = gb.T
            sums_ref[5:6, :] += jnp.sum(gb.astype(F32), 0, keepdims=True)


def attention_backward(
    x_ref, g_ref, rows_ref, dh1_ref, gb_ref, gbt_ref, q_ref, v_ref, kt_ref, p_ref,
    o_ref, a1t_ref,
    d0_ref, xg_ref, sums_ref, bqv_ref,
    do_ref, delta_ref, dqt_ref, dq_ref, dk_ref, dv_ref, da1_ref,
):
    t = pl.program_id(0)
    n = x_ref.shape[0]
    width = g_ref.shape[-1]
    heads = width // HEAD_DIM
    step = 256
    pick = (
        lax.broadcasted_iota(jnp.int32, (16, width), 1) // HEAD_DIM
        == lax.broadcasted_iota(jnp.int32, (16, width), 0)
    ).astype(BF16)

    @pl.loop(0, n // step)
    def _(b):
        rows = pl.ds(pl.multiple_of(b * step, step), step)
        do = dot_nn(gb_ref[rows, :], g_ref[0, 3]).astype(BF16)
        do_ref[rows, :] = do
        prod = do.astype(F32) * o_ref[0, rows, :].astype(F32)
        high = prod.astype(BF16)
        low = (prod - high.astype(F32)).astype(BF16)
        delta_ref[:, rows] = dot_nt(pick, high) + dot_nt(pick, low)

    dqt_ref[...] = jnp.zeros_like(dqt_ref)
    for b in range(n // step):
        first, last = b * step, (b + 1) * step
        do = do_ref[first:, :]
        q = q_ref[0, first:, :]
        v = v_ref[0, first:last, :]
        dk, dv = None, None
        for h in range(heads):
            mine = head_mask((1, width), h)
            zero = jnp.zeros((), BF16)
            p = p_ref[0, h, first:last, first:]
            dp = dot_nt(jnp.where(mine, v, zero), do)
            ds = (p.astype(F32) * (dp - delta_ref[h : h + 1, first:])).astype(BF16)
            part = dot_nn(p, jnp.where(mine, do, zero))
            dv = part if dv is None else dv + part
            part = dot_nn(ds, jnp.where(mine, q, zero))
            dk = part if dk is None else dk + part
            head = slice(h * HEAD_DIM, (h + 1) * HEAD_DIM)
            dqt_ref[head, first:] += dot_nn(kt_ref[0, head, first:last], ds)
        dk_ref[first:last, :] = dk.astype(BF16)
        dv_ref[first:last, :] = dv.astype(BF16)

    @pl.when(t == 0)
    def _():
        da1_ref[...] = jnp.zeros_like(da1_ref)

    bqv_ref[...] = jnp.zeros_like(bqv_ref)

    @pl.loop(0, n // step)
    def _(b):
        rows = pl.ds(pl.multiple_of(b * step, step), step)
        dq = (dqt_ref[:, rows] * HEAD_DIM ** -0.5).astype(BF16).T
        dk = dk_ref[rows, :]
        dv = dv_ref[rows, :]
        dq_ref[rows, :] = dq
        bqv_ref[0, 0:1, :] += jnp.sum(dq.astype(F32), 0, keepdims=True)
        bqv_ref[0, 1:2, :] += jnp.sum(dv.astype(F32), 0, keepdims=True)
        da1_ref[rows, :] += (
            dot_nt(dq, g_ref[0, 0]) + dot_nt(dk, g_ref[0, 1]) + dot_nt(dv, g_ref[0, 2])
        )

    @pl.loop(0, D // step)
    def _(b):
        rows = pl.ds(pl.multiple_of(b * step, step), step)
        a1t = a1t_ref[rows, :]
        d0_ref[0, 0, rows, :] = dot_nn(a1t, dq_ref[...]).astype(BF16)
        d0_ref[0, 1, rows, :] = dot_nn(a1t, dk_ref[...]).astype(BF16)
        d0_ref[0, 2, rows, :] = dot_nn(a1t, dv_ref[...]).astype(BF16)
        d0_ref[0, 3, rows, :] = dot_nn(gbt_ref[rows, :], o_ref[0]).astype(BF16)

    @pl.when(t == pl.num_programs(0) - 1)
    def _():
        sums_ref[...] = jnp.zeros_like(sums_ref)

        @pl.loop(0, n // step)
        def _(b):
            rows = pl.ds(pl.multiple_of(b * step, step), step)
            xhat, r = norm_parts(x_ref[rows, :].astype(F32))
            da1 = da1_ref[rows, :]
            sums_ref[0:1, :] += jnp.sum(da1 * xhat, 0, keepdims=True)
            sums_ref[1:2, :] += jnp.sum(da1, 0, keepdims=True)
            dg = da1 * rows_ref[0:1, :]
            dv = r * (
                dg
                - jnp.mean(dg, -1, keepdims=True)
                - xhat * jnp.mean(dg * xhat, -1, keepdims=True)
            )
            xg_ref[rows, :] = (dh1_ref[rows, :] + dv).astype(BF16)


def whole(*shape):
    return pl.BlockSpec(shape, lambda t: (0,) * len(shape))


def group(*shape):
    return pl.BlockSpec((1,) + shape, lambda t: (t,) + (0,) * len(shape))


def shaped(dtype, *shape):
    return jax.ShapeDtypeStruct(shape, dtype)


SMEM_WHOLE = pl.BlockSpec(memory_space=pltpu.SMEM)


def run_attention_forward(length, x, g0, rows, bqv):
    n = x.shape[0]
    groups, _, _, width = g0.shape
    heads = width // HEAD_DIM
    return pl.pallas_call(
        attention_forward,
        grid=(groups,),
        in_specs=[SMEM_WHOLE, whole(n, D), group(4, D, width), whole(16, D), group(2, width)],
        out_specs=[
            group(n, width), group(n, width), group(width, n), group(heads, n, n),
            group(n, width), whole(D, n), whole(n, D), whole(n, D), whole(D, n),
        ],
        out_shape=[
            shaped(BF16, groups, n, width), shaped(BF16, groups, n, width),
            shaped(BF16, groups, width, n), shaped(BF16, groups, heads, n, n),
            shaped(BF16, groups, n, width), shaped(BF16, D, n), shaped(F32, n, D),
            shaped(BF16, n, D), shaped(BF16, D, n),
        ],
        scratch_shapes=[
            pltpu.VMEM((n, D), BF16), pltpu.VMEM((n, width), BF16),
            pltpu.VMEM((width, n), BF16), pltpu.VMEM((width, n), BF16),
            pltpu.VMEM((n, D), F32),
        ],
        compiler_params=pltpu.CompilerParams(vmem_limit_bytes=VMEM_LIMIT),
        name="attention_forward",
    )(length, x, g0, rows, bqv)


def run_feed_forward(length, cot, a2, a2t, h1, g1, g2, rows):
    n = cot.shape[0]
    groups, _, width = g1.shape
    return pl.pallas_call(
        feed_forward_both,
        grid=(groups,),
        in_specs=[
            SMEM_WHOLE, whole(n, D), whole(n, D), whole(D, n), whole(n, D),
            group(D, width), group(D, width), whole(16, D),
        ],
        out_specs=[
            whole(n, D), group(D, width), group(D, width), whole(n, D), whole(n, D),
            whole(D, n), whole(16, D),
        ],
        out_shape=[
            shaped(BF16, n, D), shaped(BF16, groups, D, width), shaped(BF16, groups, D, width),
            shaped(F32, n, D), shaped(BF16, n, D), shaped(BF16, D, n), shaped(F32, 16, D),
        ],
        scratch_shapes=[
            pltpu.VMEM((n, D), BF16), pltpu.VMEM((D, n), BF16), pltpu.VMEM((n, D), F32),
            pltpu.VMEM((n, D), F32), pltpu.VMEM((n, width), BF16), pltpu.VMEM((n, width), BF16),
        ],
        compiler_params=pltpu.CompilerParams(vmem_limit_bytes=VMEM_LIMIT),
        name="feed_forward_both",
    )(length, cot, a2, a2t, h1, g1, g2, rows)


def run_attention_backward(x, g0, rows, dh1, gb, gbt, q, v, kt, p, o, a1t):
    n = x.shape[0]
    groups, _, _, width = g0.shape
    heads = width // HEAD_DIM
    return pl.pallas_call(
        attention_backward,
        grid=(groups,),
        in_specs=[
            whole(n, D), group(4, D, width), whole(16, D), whole(n, D), whole(n, D),
            whole(D, n), group(n, width), group(n, width), group(width, n),
            group(heads, n, n), group(n, width), whole(D, n),
        ],
        out_specs=[group(4, D, width), whole(n, D), whole(8, D), group(8, width)],
        out_shape=[
            shaped(BF16, groups, 4, D, width), shaped(BF16, n, D), shaped(F32, 8, D),
            shaped(F32, groups, 8, width),
        ],
        scratch_shapes=[
            pltpu.VMEM((n, width), BF16), pltpu.VMEM((16, n), F32), pltpu.VMEM((width, n), F32),
            pltpu.VMEM((n, width), BF16), pltpu.VMEM((n, width), BF16),
            pltpu.VMEM((n, width), BF16), pltpu.VMEM((n, D), F32),
        ],
        compiler_params=pltpu.CompilerParams(vmem_limit_bytes=VMEM_LIMIT),
        name="attention_backward",
    )(x, g0, rows, dh1, gb, gbt, q, v, kt, p, o, a1t)


Z_DEV, Y_DEV, X_DEV, C_DEV = 4, 2, 2, 2


class Place:
    def __init__(self):
        dp, self.t = lax.axis_index("dp"), lax.axis_index("tensor")
        self.dp = dp
        self.z, self.y = dp // 2, dp % 2
        self.x, self.c = self.t // 2, self.t % 2
        self.other_y = 1 - self.y
        self.zs = [
            self.z,
            self.z + 1 - 2 * (self.z % 2),
            self.z + 2 - 4 * (self.z // 2),
            3 - self.z,
        ]
        self.ts = [
            self.t,
            self.t + 1 - 2 * (self.t % 2),
            self.t + 2 - 4 * (self.t // 2),
            3 - self.t,
        ]
        self.to_z = [dict(dp=z * 2 + self.y) for z in self.zs]
        self.to_y = dict(dp=self.z * 2 + self.other_y)
        self.to_x = dict(tensor=self.ts[2])
        self.to_core = dict(tensor=self.ts[1])

    def group(self, k):
        return lax.select(
            k == 0, self.ts[0],
            lax.select(k == 1, self.ts[1], lax.select(k == 2, self.ts[2], self.ts[3])),
        )

    def greet(self):
        barrier = pltpu.get_barrier_semaphore()
        others = self.to_z[1:] + [self.to_y, self.to_x, self.to_core]
        for device in others:
            pl.semaphore_signal(
                barrier, inc=1, device_id=device, device_id_type=pl.DeviceIdType.MESH
            )
        pl.semaphore_wait(barrier, len(others))


class Links:
    def __init__(self, send_sem, recv_sem):
        self.send_sem, self.recv_sem = send_sem, recv_sem
        self.copies = []

    def add(self, device, src, dst):
        number = len(self.copies)
        copy = pltpu.make_async_remote_copy(
            src_ref=src,
            dst_ref=dst,
            send_sem=self.send_sem.at[number],
            recv_sem=self.recv_sem.at[number],
            device_id=device,
            device_id_type=pl.DeviceIdType.MESH,
        )
        self.copies.append(copy)
        return copy

    def sent(self):
        for copy in self.copies:
            copy.wait_send()


def flat(copies):
    for item in copies:
        if isinstance(item, list):
            yield from flat(item)
        else:
            yield item


def start(*copies):
    for copy in flat(copies):
        copy.start()


def recv(*copies):
    for copy in flat(copies):
        copy.wait_recv()


class Gather:
    def __init__(self, links, place, own, full, y_first):
        every = slice(None)
        y, other = place.y, place.other_y
        first = place.to_y if y_first else place.to_x
        second = place.to_x if y_first else place.to_y
        shift = 0 if y_first else 2
        self.z = [
            links.add(place.to_z[k], own, full(0, place.z, y)) for k in range(1, 4)
        ]
        self.first = [links.add(first, own, full(shift, place.z, y))]
        for k in range(1, 4):
            z = place.zs[k]
            self.first.append(links.add(first, full(0, z, y), full(shift, z, y)))
        if y_first:
            second_blocks = [((0, y), (2, y)), ((0, other), (2, other))]
            core_blocks = [(0, y), (0, other), (2, y), (2, other)]
        else:
            second_blocks = [((0, y), (0, y)), ((2, y), (2, y))]
            core_blocks = [(0, y), (2, y), (0, other), (2, other)]
        self.second = [
            links.add(second, full(k, every, yy), full(to, every, to_y))
            for (k, yy), (to, to_y) in second_blocks
        ]
        self.core = [
            links.add(place.to_core, full(k, every, yy), full(k + 1, every, yy))
            for k, yy in core_blocks
        ]


def fused_forward(
    len_ref, x_ref, own0_ref, own1_ref, own2_ref, vec_ref,
    g_ref, w1_ref, w2_ref, rows_ref,
    q_ref, v_ref, kt_ref, p_ref, o_ref, a1t_ref, h1_ref, a2_ref, a2t_ref,
    all_ref, vecs_ref, bqv_ref, a1_ref, k_ref, vt_ref, ot_ref, attn_ref,
    send_sem, recv_sem, local_sem,
):
    t = pl.program_id(0)
    n = x_ref.shape[0]
    width = all_ref.shape[-1]
    heads = width // HEAD_DIM
    step = 256
    length = len_ref[0]
    place = Place()
    links = Links(send_sem, recv_sem)
    z, y, x, c = place.z, place.y, place.x, place.c
    vec_z = [
        links.add(place.to_z[k], vec_ref, vecs_ref.at[z, y, x, c]) for k in range(1, 4)
    ]
    vec_y = links.add(place.to_y, vecs_ref.at[:, y, x, c], vecs_ref.at[:, y, x, c])
    vec_x = links.add(place.to_x, vecs_ref.at[:, :, x, c], vecs_ref.at[:, :, x, c])
    vec_core = links.add(place.to_core, vecs_ref.at[:, :, :, c], vecs_ref.at[:, :, :, c])
    seg0 = Gather(links, place, own0_ref, lambda k, z, y: all_ref.at[k, :, z, y], True)
    seg1 = Gather(links, place, own1_ref, lambda k, z, y: w1_ref.at[k, z, y], False)
    seg2 = Gather(links, place, own2_ref, lambda k, z, y: w2_ref.at[k, z, y], False)
    keep1 = pltpu.make_async_copy(own1_ref, w1_ref.at[0, z, y], local_sem.at[0])
    keep2 = pltpu.make_async_copy(own2_ref, w2_ref.at[0, z, y], local_sem.at[1])

    def serve(now, *acts):
        @pl.when(t == now)
        def _():
            for act, *copies in acts:
                act(*copies)

    @pl.when(t == 0)
    def _():
        place.greet()
        start(vec_z, seg0.z[1], seg0.z[2], seg0.z[0], seg0.first[0])
        vecs_ref[z, y, x, c] = vec_ref[...]
        all_ref[0, :, z, y] = own0_ref[...]
        keep1.start()
        keep2.start()
        recv(vec_z)
        start(vec_y)
        recv(seg0.z[0])
        start(seg0.first[1])
        recv(vec_y)
        start(vec_x)
        recv(vec_x)
        start(vec_core)
        recv(seg0.z[1])
        start(seg0.first[2])
        recv(vec_core)
        vecs = vecs_ref[...].reshape(D, vecs_ref.shape[-1]).T[:16]
        rows_ref[...] = vecs
        for group in range(4):
            bqv_ref[group, 0:2, :] = vecs[3:5, group * width : (group + 1) * width]

        @pl.loop(0, n // step)
        def _(b):
            rows = pl.ds(pl.multiple_of(b * step, step), step)
            wide = x_ref[rows, :].astype(F32)
            xhat, _ = norm_parts(wide)
            a1 = (xhat * rows_ref[0:1, :] + rows_ref[2:3, :]).astype(BF16)
            a1_ref[rows, :] = a1
            a1t_ref[:, rows] = a1.T
            attn_ref[rows, :] = wide + rows_ref[5:6, :]

        recv(seg0.z[2])
        start(seg0.first[3], seg0.second[0], seg0.core[0])
        recv(seg0.first)
        start(seg0.second[1], seg0.core[1])
        keep1.wait()
        keep2.wait()
        start(seg1.z[1], seg1.z[2], seg1.z[0], seg1.first[0], seg2.z[1], seg2.z[2], seg2.z[0], seg2.first[0])

    serve(1, (recv, seg0.core[0], seg0.core[1]))
    serve(2, (recv, seg0.second[0], seg0.second[1]))
    serve(3, (recv, seg0.core[2], seg0.core[3]))

    g_ref[0] = all_ref[t].reshape(g_ref.shape[1:])
    mine = place.group(t)

    @pl.loop(0, n // step)
    def _(b):
        rows = pl.ds(pl.multiple_of(b * step, step), step)
        a1 = a1_ref[rows, :]
        q = (dot_nn(a1, g_ref[0, 0]) + bqv_ref[mine, 0:1, :]).astype(BF16)
        q_ref[0, rows, :] = q * jnp.asarray(HEAD_DIM ** -0.5, BF16)
        k = dot_nn(a1, g_ref[0, 1]).astype(BF16)
        k_ref[rows, :] = k
        kt_ref[0, :, rows] = k.T
        v = (dot_nn(a1, g_ref[0, 2]) + bqv_ref[mine, 1:2, :]).astype(BF16)
        v_ref[0, rows, :] = v
        vt_ref[:, rows] = v.T

    for h in range(heads):
        if h == 0:
            serve(0, (recv, seg1.z), (start, seg1.first[1:], seg1.second[0], seg1.core[0]))
            serve(2, (start, seg0.core[2], seg0.core[3]), (recv, seg1.second[0]), (start, seg1.core[2]))
        if h == 1:
            serve(0, (recv, seg2.z), (start, seg2.first[1:], seg2.second[0], seg2.core[0]))
            serve(1, (recv, seg1.first), (start, seg1.second[1], seg1.core[1]))
            serve(3, (recv, seg2.second[0]), (start, seg2.core[2]))
        if h == 2:
            serve(1, (recv, seg2.first), (start, seg2.second[1], seg2.core[1]))
            serve(3, (recv, seg1.second[1]), (start, seg1.core[3]))
        k = k_ref[...]
        k = jnp.where(head_mask(k.shape, h), k, jnp.zeros_like(k))
        for b in range(n // step):
            first, last = b * step, (b + 1) * step
            q = q_ref[0, first:last, :]
            key = lax.broadcasted_iota(jnp.int32, (last, step), 0)
            query = lax.broadcasted_iota(jnp.int32, (step, step), 1) + first
            s = dot_nt(k[:last], q)
            near = jnp.where(
                (key[first:] <= query) & (key[first:] < length), s[first:], MASKED
            )
            if b:
                far = jnp.where(key[:first] < length, s[:first], MASKED)
                top = jnp.maximum(
                    jnp.max(far, 0, keepdims=True), jnp.max(near, 0, keepdims=True)
                )
                e_far = jnp.exp(far - top)
                e_near = jnp.exp(near - top)
                total = jnp.sum(e_far, 0, keepdims=True) + jnp.sum(e_near, 0, keepdims=True)
                scale = 1.0 / total
                p_ref[0, h, :first, first:last] = (e_far * scale).astype(BF16)
            else:
                top = jnp.max(near, 0, keepdims=True)
                e_near = jnp.exp(near - top)
                scale = 1.0 / jnp.sum(e_near, 0, keepdims=True)
            p_ref[0, h, first:last, first:last] = (e_near * scale).astype(BF16)
            ot_ref[h * HEAD_DIM : (h + 1) * HEAD_DIM, first:last] = dot_nn(
                vt_ref[h * HEAD_DIM : (h + 1) * HEAD_DIM, :last],
                p_ref[0, h, :last, first:last],
            ).astype(BF16)

    @pl.loop(0, n // step)
    def _(b):
        rows = pl.ds(pl.multiple_of(b * step, step), step)
        o = ot_ref[:, rows].T
        o_ref[0, rows, :] = o
        attn_ref[rows, :] += dot_nt(o, g_ref[0, 3])

    @pl.when(t == pl.num_programs(0) - 1)
    def _():
        @pl.loop(0, n // step)
        def _(b):
            rows = pl.ds(pl.multiple_of(b * step, step), step)
            h1 = attn_ref[rows, :]
            h1_ref[rows, :] = h1
            xhat, _ = norm_parts(h1)
            a2 = (xhat * rows_ref[1:2, :] + rows_ref[6:7, :]).astype(BF16)
            a2_ref[rows, :] = a2
            a2t_ref[:, rows] = a2.T

        recv(seg2.second[1])
        start(seg2.core[3])
        recv(seg1.core, seg2.core)
        links.sent()


N_GATHER = 6 + 3 * 13
VMEM_WHOLE = pl.BlockSpec(memory_space=pltpu.VMEM)
ANY_WHOLE = pl.BlockSpec(memory_space=pl.ANY)


def run_fused_forward(length, x, own0, own1, own2, vec):
    n = x.shape[0]
    groups = 4
    _, depth, width = own0.shape
    heads = width // HEAD_DIM
    hidden = own1.shape[1]
    return pl.pallas_call(
        fused_forward,
        grid=(groups,),
        in_specs=[SMEM_WHOLE] + [VMEM_WHOLE] * 5,
        out_specs=[
            group(4, D, width), ANY_WHOLE, ANY_WHOLE, whole(16, D),
            group(n, width), group(n, width), group(width, n), group(heads, n, n),
            group(n, width), whole(D, n), whole(n, D), whole(n, D), whole(D, n),
        ],
        out_shape=[
            shaped(BF16, groups, 4, D, width),
            shaped(BF16, groups, Z_DEV, Y_DEV, depth, hidden),
            shaped(BF16, groups, Z_DEV, Y_DEV, depth, hidden),
            shaped(F32, 16, D),
            shaped(BF16, groups, n, width), shaped(BF16, groups, n, width),
            shaped(BF16, groups, width, n), shaped(BF16, groups, heads, n, n),
            shaped(BF16, groups, n, width), shaped(BF16, D, n), shaped(F32, n, D),
            shaped(BF16, n, D), shaped(BF16, D, n),
        ],
        scratch_shapes=[
            pltpu.VMEM((groups, 4, Z_DEV, Y_DEV, depth, width), BF16),
            pltpu.VMEM((Z_DEV, Y_DEV, X_DEV, C_DEV) + vec.shape, F32),
            pltpu.VMEM((groups, 8, width), F32),
            pltpu.VMEM((n, D), BF16), pltpu.VMEM((n, width), BF16),
            pltpu.VMEM((width, n), BF16), pltpu.VMEM((width, n), BF16),
            pltpu.VMEM((n, D), F32),
            pltpu.SemaphoreType.DMA((N_GATHER,)), pltpu.SemaphoreType.DMA((N_GATHER,)),
            pltpu.SemaphoreType.DMA((2,)),
        ],
        compiler_params=pltpu.CompilerParams(
            vmem_limit_bytes=VMEM_LIMIT, collective_id=0, has_side_effects=True
        ),
        name="fused_forward",
    )(length, x, own0, own1, own2, vec)


def group_order(i):
    return (1 + 2 * i) % 4 - i // 2


def fused_feed_forward(
    len_ref, c_ref, a2_ref, a2t_ref, h1_ref, w1_ref, w2_ref, rows_ref,
    out_ref, d1_ref, d2_ref, dh1_ref, gb_ref, gbt_ref, sums_ref,
    gf_ref, gft_ref, feed_ref, da2_ref, h_ref, slope_ref,
    stage1_ref, land1_ref, stage2_ref, land2_ref, work2_ref, cross2_ref, own_ref,
    send_sem, recv_sem, local_sem,
):
    t = pl.program_id(0)
    n = c_ref.shape[0]
    step = 256
    depth = stage2_ref.shape[-2]
    length = len_ref[0]
    place = Place()
    links = Links(send_sem, recv_sem)
    y, other = place.y, place.other_y
    quarter = n // 4
    core2 = [links.add(place.to_core, stage2_ref.at[i], land2_ref.at[i]) for i in range(2)]
    core1 = [links.add(place.to_core, stage1_ref.at[i], land1_ref.at[i]) for i in range(2)]
    cross2 = [
        links.add(place.to_y, work2_ref.at[i, :, other], cross2_ref.at[i]) for i in range(2)
    ]
    out_x, out_core, out_far = [], [], []
    for i in range(4):
        rows = pl.ds(i * quarter, quarter)
        mine_there = out_ref.at[place.t, rows]
        far = out_ref.at[place.ts[2], rows]
        out_x.append(links.add(place.to_x, own_ref.at[rows], mine_there))
        out_core.append(links.add(place.to_core, own_ref.at[rows], mine_there))
        out_far.append(links.add(place.to_core, far, far))
    keep = pltpu.make_async_copy(own_ref, out_ref.at[place.t], local_sem)
    k = group_order(t % 4)
    mine = place.group(k)

    def weight_grad(left_ref, right, put):
        @pl.loop(0, Z_DEV)
        def _(z):
            rows = pl.ds(pl.multiple_of(z * Y_DEV * depth, Y_DEV * depth), Y_DEV * depth)
            value = dot_nn(left_ref[rows, :], right())
            put(z, value.reshape(Y_DEV, depth, value.shape[-1]))

    @pl.when(t == 0)
    def _():
        place.greet()
        sums_ref[...] = jnp.zeros_like(sums_ref)

        @pl.loop(0, n // step)
        def _(b):
            rows = pl.ds(pl.multiple_of(b * step, step), step)
            at = b * step + lax.broadcasted_iota(jnp.int32, (step, 1), 0)
            live = (at < length).astype(F32)
            g = (c_ref[rows, :].astype(F32) * live).astype(BF16)
            gf_ref[rows, :] = g
            gft_ref[:, rows] = g.T
            sums_ref[7:8, :] += jnp.sum(g.astype(F32), 0, keepdims=True)

    @pl.when(t < 4)
    def _():
        bias = rows_ref[pl.ds(8 + mine, 1), :]

        @pl.loop(0, n // step)
        def _(b):
            rows = pl.ds(pl.multiple_of(b * step, step), step)
            f = dot_nn(a2_ref[rows, :], w1_ref[0]) + bias
            f2 = f * f
            th = jnp.tanh(f * (SQRT_2_PI + (SQRT_2_PI * 0.044715) * f2))
            half = 0.5 + 0.5 * th
            h = (f * half).astype(BF16)
            slope = half + f * (0.5 - 0.5 * th * th) * (
                SQRT_2_PI + (3 * SQRT_2_PI * 0.044715) * f2
            )
            h_ref[k, rows, :] = h
            slope_ref[k, rows, :] = slope.astype(BF16)
            feed = dot_nt(h, w2_ref[0])

            @pl.when(t == 0)
            def _():
                feed_ref[rows, :] = feed

            @pl.when(t > 0)
            def _():
                feed_ref[rows, :] += feed

    @pl.when(t < 2)
    def _():
        def put(z, value):
            stage2_ref[t, z] = value.astype(BF16)

        weight_grad(gft_ref, lambda: h_ref[k], put)
        for i in range(2):
            @pl.when(t == i)
            def _():
                start(core2[i])

    @pl.when(t == 3)
    def _():
        @pl.loop(0, n // step)
        def _(b):
            rows = pl.ds(pl.multiple_of(b * step, step), step)
            at = b * step + lax.broadcasted_iota(jnp.int32, (step, 1), 0)
            live = (at < length).astype(F32)
            own_ref[rows, :] = (
                live * (h1_ref[rows, :] + (feed_ref[rows, :] + rows_ref[7:8, :]))
            ).astype(BF16)

        for i in range(4):
            start(out_x[i])
        for i in range(4):
            start(out_core[i])
        keep.start()

    @pl.when((t == 4) | (t == 5))
    def _():
        for i in range(2):
            @pl.when(t == 4 + i)
            def _():
                recv(core2[i])

        def put(z, value):
            work2_ref[t - 4, z] = (value + land2_ref[t - 4, z].astype(F32)).astype(BF16)

        weight_grad(gft_ref, lambda: h_ref[2 * (t - 4)], put)
        for i in range(2):
            @pl.when(t == 4 + i)
            def _():
                start(cross2[i])

    @pl.when(t >= 4)
    def _():
        @pl.loop(0, n // step)
        def _(b):
            rows = pl.ds(pl.multiple_of(b * step, step), step)
            dh = dot_nn(gf_ref[rows, :], w2_ref[0])
            df = (dh * slope_ref[k, rows, :].astype(F32)).astype(BF16)
            slope_ref[k, rows, :] = df
            sums_ref[pl.ds(8 + mine, 1), :] += jnp.sum(df.astype(F32), 0, keepdims=True)
            da2 = dot_nt(df, w1_ref[0])

            @pl.when(t == 4)
            def _():
                da2_ref[rows, :] = da2

            @pl.when(t > 4)
            def _():
                da2_ref[rows, :] += da2

    @pl.when((t == 4) | (t == 5))
    def _():
        def put(z, value):
            stage1_ref[t - 4, z] = value.astype(BF16)

        weight_grad(a2t_ref, lambda: slope_ref[k], put)
        for i in range(2):
            @pl.when(t == 4 + i)
            def _():
                start(core1[i])

    @pl.when(t >= 6)
    def _():
        for i in range(2):
            @pl.when(t == 6 + i)
            def _():
                recv(core1[i])
                recv(out_x[i])
                start(out_far[i])

        def put(z, value):
            d1_ref[t - 6, z] = (value + land1_ref[t - 6, z].astype(F32)).astype(BF16)

        weight_grad(a2t_ref, lambda: slope_ref[k], put)

    @pl.when(t == 7)
    def _():
        @pl.loop(0, n // step)
        def _(b):
            rows = pl.ds(pl.multiple_of(b * step, step), step)
            at = b * step + lax.broadcasted_iota(jnp.int32, (step, 1), 0)
            live = (at < length).astype(F32)
            xhat, r = norm_parts(h1_ref[rows, :])
            da2 = da2_ref[rows, :]
            sums_ref[1:2, :] += jnp.sum(da2 * xhat, 0, keepdims=True)
            sums_ref[6:7, :] += jnp.sum(da2, 0, keepdims=True)
            dg = da2 * rows_ref[1:2, :]
            dv = r * (
                dg
                - jnp.mean(dg, -1, keepdims=True)
                - xhat * jnp.mean(dg * xhat, -1, keepdims=True)
            )
            dh1 = live * c_ref[rows, :].astype(F32) + dv
            dh1_ref[rows, :] = dh1
            gb = dh1.astype(BF16)
            gb_ref[rows, :] = gb
            gbt_ref[:, rows] = gb.T
            sums_ref[5:6, :] += jnp.sum(gb.astype(F32), 0, keepdims=True)

        recv(cross2[0], cross2[1])

        @pl.loop(0, Z_DEV)
        def _(z):
            for i in range(2):
                d2_ref[i, z] = (
                    work2_ref[i, z, y].astype(F32) + cross2_ref[i, z].astype(F32)
                ).astype(BF16)

        for i in range(2, 4):
            recv(out_x[i])
            start(out_far[i])
        for i in range(4):
            recv(out_core[i], out_far[i])
        links.sent()
        keep.wait()


def fused_backward(
    x_ref, g_ref, rows_ref, dh1_ref, gb_ref, gbt_ref, q_ref, v_ref, kt_ref, p_ref,
    o_ref, a1t_ref, d1_ref, d2_ref, early_ref,
    out_ref, part0_ref, part1_ref, part2_ref, total_ref,
    do_ref, delta_ref, dqt_ref, dq_ref, dk_ref, dv_ref, da1_ref, own_ref, bqv_ref,
    work1_ref, cross1_ref, side1_ref, far1_ref,
    work2_ref, side2_ref, far2_ref,
    stagew_ref, landw_ref, workw_ref, crossw_ref, sidew_ref, farw_ref,
    stage0_ref, land0_ref, work0_ref, cross0_ref, crossk_ref, side0_ref, far0_ref,
    sums_ref, sumland_ref,
    send_sem, recv_sem, local_sem,
):
    t = pl.program_id(0)
    n = x_ref.shape[0]
    width = g_ref.shape[-1]
    depth = part0_ref.shape[1]
    heads = width // HEAD_DIM
    step = n // 4
    place = Place()
    links = Links(send_sem, recv_sem)
    z, y, other = place.z, place.y, place.other_y
    b = t // 4
    k = group_order(t % 4)
    mine = place.group(k)
    out_x, out_core, out_far = [], [], []
    for i in range(4):
        rows = pl.ds(i * step, step)
        mine_there = out_ref.at[place.t, rows]
        far = out_ref.at[place.ts[2], rows]
        out_x.append(links.add(place.to_x, own_ref.at[rows], mine_there))
        out_core.append(links.add(place.to_core, own_ref.at[rows], mine_there))
        out_far.append(links.add(place.to_core, far, far))
    keeps = [
        pltpu.make_async_copy(
            own_ref.at[pl.ds(i * step, step)],
            out_ref.at[place.t, pl.ds(i * step, step)],
            local_sem.at[i],
        )
        for i in range(4)
    ]
    def to_owners(block, far_ref):
        return [
            links.add(place.to_z[i], block(place.zs[i]), far_ref.at[i - 1])
            for i in range(1, 4)
        ]

    cross1 = links.add(place.to_y, d1_ref.at[:, :, other], cross1_ref)
    side1 = links.add(place.to_x, work1_ref.at[1], side1_ref)
    far1 = to_owners(lambda i: work1_ref.at[0, i], far1_ref)
    side2 = links.add(place.to_x, d2_ref.at[1], side2_ref)
    far2 = to_owners(lambda i: work2_ref.at[i], far2_ref)
    corew = [links.add(place.to_core, stagew_ref.at[i], landw_ref.at[i]) for i in range(2)]
    crossw = links.add(place.to_y, workw_ref.at[:, :, other], crossw_ref)
    sidew = links.add(place.to_x, workw_ref.at[1, :, y], sidew_ref)
    farw = to_owners(lambda i: workw_ref.at[0, i, y], farw_ref)
    core0 = [
        [
            links.add(place.to_core, stage0_ref.at[i, j], land0_ref.at[i, j])
            for i in range(2)
        ]
        for j in range(3)
    ]
    cross0 = [
        links.add(place.to_x, work0_ref.at[1, j], crossk_ref)
        if j == 1
        else links.add(place.to_y, work0_ref.at[:, j, :, other], cross0_ref.at[j // 2])
        for j in range(3)
    ]
    side0 = [
        links.add(place.to_y, work0_ref.at[0, j, :, other], side0_ref.at[j])
        if j == 1
        else links.add(place.to_x, work0_ref.at[1, j, :, y], side0_ref.at[j])
        for j in range(3)
    ]
    far0 = [
        to_owners(lambda i, j=j: work0_ref.at[0, j, i, y], far0_ref.at[j]) for j in range(3)
    ]
    sum_core, sum_x, sum_y, *sum_z = [
        links.add(to, sums_ref.at[min(i, 3)], sumland_ref.at[i])
        for i, to in enumerate([place.to_core, place.to_x, place.to_y] + place.to_z[1:])
    ]

    def add(target, left, right):
        target[...] = (left[...].astype(F32) + right[...].astype(F32)).astype(BF16)

    def when(now):
        return pl.when(t == now)

    @when(0)
    def _():
        place.greet()
        start(side2, cross1)
        bqv_ref[...] = jnp.zeros_like(bqv_ref)

    @when(3)
    def _():
        recv(side2)

        @pl.loop(0, Z_DEV)
        def _(i):
            add(work2_ref.at[i], d2_ref.at[0, i], side2_ref.at[i])

        start(far2)

    @when(6)
    def _():
        recv(cross1)

        @pl.loop(0, Z_DEV)
        def _(i):
            for s in range(2):
                add(work1_ref.at[s, i], d1_ref.at[s, i, y], cross1_ref.at[s, i])

        start(side1)
        recv(crossw)

        @pl.loop(0, Z_DEV)
        def _(i):
            for s in range(2):
                add(workw_ref.at[s, i, y], workw_ref.at[s, i, y], crossw_ref.at[s, i])

        start(sidew)

    @when(8)
    def _():
        recv(out_x[0])
        start(out_far[0])

    @when(10)
    def _():
        recv(side1)

        @pl.loop(0, Z_DEV)
        def _(i):
            add(work1_ref.at[0, i], work1_ref.at[0, i], side1_ref.at[i])

        start(far1)
        recv(sidew)

        @pl.loop(0, Z_DEV)
        def _(i):
            add(workw_ref.at[0, i, y], workw_ref.at[0, i, y], sidew_ref.at[i])

        start(farw)
        recv(far2)
        part2_ref[...] = work2_ref[z].astype(F32) + (
            far2_ref[0].astype(F32) + far2_ref[1].astype(F32) + far2_ref[2].astype(F32)
        )

    @when(12)
    def _():
        recv(out_x[1])
        start(out_far[1])

    @when(15)
    def _():
        recv(out_x[2])
        start(out_far[2])

    @pl.when(b == 0)
    def _():
        pick = (
            lax.broadcasted_iota(jnp.int32, (16, width), 1) // HEAD_DIM
            == lax.broadcasted_iota(jnp.int32, (16, width), 0)
        ).astype(BF16)

        @pl.loop(0, n // step)
        def _(i):
            rows = pl.ds(pl.multiple_of(i * step, step), step)
            do = dot_nn(gb_ref[rows, :], g_ref[0, 3]).astype(BF16)
            do_ref[k, rows, :] = do
            prod = do.astype(F32) * o_ref[0, rows, :].astype(F32)
            high = prod.astype(BF16)
            low = (prod - high.astype(F32)).astype(BF16)
            delta_ref[k, :, rows] = dot_nt(pick, high) + dot_nt(pick, low)

        dqt_ref[k] = jnp.zeros(dqt_ref.shape[1:], F32)
        for i in range(2):
            @when(2 + i)
            def _():
                recv(corew[i])

        @pl.loop(0, Z_DEV)
        def _(i):
            rows = pl.ds(pl.multiple_of(i * Y_DEV * depth, Y_DEV * depth), Y_DEV * depth)
            value = dot_nn(gbt_ref[rows, :], o_ref[0]).reshape(Y_DEV, depth, width)

            @pl.when(t < 2)
            def _():
                stagew_ref[t, i] = value.astype(BF16)

            @pl.when(t >= 2)
            def _():
                workw_ref[t - 2, i] = (value + landw_ref[t - 2, i].astype(F32)).astype(BF16)

        for i in range(2):
            @when(i)
            def _():
                start(corew[i])

        @when(3)
        def _():
            start(crossw)

    for bb in range(4):
        @pl.when(b == bb)
        def _():
            first, last = bb * step, (bb + 1) * step
            do = do_ref[k, first:, :]
            q = q_ref[0, first:, :]
            v = v_ref[0, first:last, :]
            dk, dv = None, None
            for h in range(heads):
                lanes = head_mask((1, width), h)
                zero = jnp.zeros((), BF16)
                p = p_ref[0, h, :, first:]
                dp = dot_nt(jnp.where(lanes, v, zero), do)
                ds = (p.astype(F32) * (dp - delta_ref[k, h : h + 1, first:])).astype(BF16)
                part = dot_nn(p, jnp.where(lanes, do, zero))
                dv = part if dv is None else dv + part
                part = dot_nn(ds, jnp.where(lanes, q, zero))
                dk = part if dk is None else dk + part
                head = slice(h * HEAD_DIM, (h + 1) * HEAD_DIM)
                dqt_ref[k, head, first:] += dot_nn(kt_ref[0, head, first:last], ds)
            dk = dk.astype(BF16)
            dv = dv.astype(BF16)
            dq = (dqt_ref[k, :, first:last] * HEAD_DIM ** -0.5).astype(BF16).T
            dq_ref[k, first:last, :] = dq
            dk_ref[k, first:last, :] = dk
            dv_ref[k, first:last, :] = dv
            bqv_ref[mine, 0:1, :] += jnp.sum(dq.astype(F32), 0, keepdims=True)
            bqv_ref[mine, 1:2, :] += jnp.sum(dv.astype(F32), 0, keepdims=True)
            da1 = (
                dot_nt(dq, g_ref[0, 0]) + dot_nt(dk, g_ref[0, 1]) + dot_nt(dv, g_ref[0, 2])
            )

            @pl.when(t % 4 == 0)
            def _():
                da1_ref[...] = da1

            @pl.when(t % 4 > 0)
            def _():
                da1_ref[...] += da1

    @when(0)
    def _():
        sums_ref[0] = early_ref[...]

    @pl.when(t % 4 == 3)
    def _():
        rows = pl.ds(pl.multiple_of(b * step, step), step)
        xhat, r = norm_parts(x_ref[rows, :].astype(F32))
        da1 = da1_ref[...]
        sums_ref[0, 0:1, :] += jnp.sum(da1 * xhat, 0, keepdims=True)
        sums_ref[0, 2:3, :] += jnp.sum(da1, 0, keepdims=True)
        dg = da1 * rows_ref[0:1, :]
        dv = r * (
            dg
            - jnp.mean(dg, -1, keepdims=True)
            - xhat * jnp.mean(dg * xhat, -1, keepdims=True)
        )
        own_ref[rows, :] = (dh1_ref[rows, :] + dv).astype(BF16)
        for i in range(4):
            @pl.when(b == i)
            def _():
                start(out_x[i], out_core[i])
                keeps[i].start()

    @when(15)
    def _():
        for s in range(4):
            sums_ref[0, 3:5, s * width : (s + 1) * width] = bqv_ref[s, 0:2, :]
        start(sum_core)

        def weight_grad(group, j, put):
            grad = (dq_ref, dk_ref, dv_ref)[j]

            @pl.loop(0, Z_DEV)
            def _(i):
                rows = pl.ds(pl.multiple_of(i * Y_DEV * depth, Y_DEV * depth), Y_DEV * depth)
                value = dot_nn(a1t_ref[rows, :], grad[group]).reshape(Y_DEV, depth, width)
                put(i, value)

        for j in range(3):
            for s in range(2):
                def put(i, value):
                    stage0_ref[s, j, i] = value.astype(BF16)

                weight_grad(2 * s + 1, j, put)
                start(core0[j][s])
        for j in range(3):
            for s in range(2):
                recv(core0[j][s])

                def put(i, value):
                    work0_ref[s, j, i] = (value + land0_ref[s, j, i].astype(F32)).astype(BF16)

                weight_grad(2 * s, j, put)
            start(cross0[j])
        recv(sum_core)
        sums_ref[1] = sums_ref[0] + sumland_ref[0]
        start(sum_x)
        recv(far1)
        part1_ref[...] = work1_ref[0, z].astype(F32) + (
            far1_ref[0].astype(F32) + far1_ref[1].astype(F32) + far1_ref[2].astype(F32)
        )
        recv(farw)
        part0_ref[3] = workw_ref[0, z, y].astype(F32) + (
            farw_ref[0].astype(F32) + farw_ref[1].astype(F32) + farw_ref[2].astype(F32)
        )
        recv(sum_x)
        sums_ref[2] = sums_ref[1] + sumland_ref[1]
        start(sum_y)
        for j in range(3):
            recv(cross0[j])

            @pl.loop(0, Z_DEV)
            def _(i):
                if j == 1:
                    add(work0_ref.at[0, j, i], work0_ref.at[0, j, i], crossk_ref.at[i])
                else:
                    for s in range(2):
                        add(
                            work0_ref.at[s, j, i, y], work0_ref.at[s, j, i, y],
                            cross0_ref.at[j // 2, s, i],
                        )

            start(side0[j])
            if j == 0:
                recv(sum_y)
                sums_ref[3] = sums_ref[2] + sumland_ref[2]
                start(sum_z)
        for j in range(3):
            recv(side0[j])

            @pl.loop(0, Z_DEV)
            def _(i):
                add(work0_ref.at[0, j, i, y], work0_ref.at[0, j, i, y], side0_ref.at[j, i])

            start(far0[j])
        recv(out_x[3])
        start(out_far[3])
        recv(sum_z)
        total_ref[...] = (sums_ref[3] + sumland_ref[3]) + (sumland_ref[4] + sumland_ref[5])
        for j in range(3):
            recv(far0[j])
            part0_ref[j] = work0_ref[0, j, z, y].astype(F32) + (
                far0_ref[j, 0].astype(F32)
                + far0_ref[j, 1].astype(F32)
                + far0_ref[j, 2].astype(F32)
            )
        for i in range(4):
            recv(out_core[i], out_far[i])
            keeps[i].wait()
        links.sent()


def run_fused_feed_forward(length, cot, a2, a2t, h1, g1, g2, rows):
    n = cot.shape[0]
    groups, hidden = g1.shape[0], g1.shape[-1]
    depth = D // (Z_DEV * Y_DEV)
    halves = (2, Z_DEV, Y_DEV, depth, hidden)
    weight = pl.BlockSpec((1, D, hidden), lambda t: (group_order(t % 4), 0, 0))
    return pl.pallas_call(
        fused_feed_forward,
        grid=(2 * groups,),
        in_specs=[SMEM_WHOLE] + [VMEM_WHOLE] * 4 + [weight, weight, VMEM_WHOLE],
        out_specs=[ANY_WHOLE] + [VMEM_WHOLE] * 6,
        out_shape=[
            shaped(BF16, groups, n, D), shaped(BF16, *halves),
            shaped(BF16, 2, Z_DEV, depth, hidden), shaped(F32, n, D), shaped(BF16, n, D),
            shaped(BF16, D, n), shaped(F32, 16, D),
        ],
        scratch_shapes=[
            pltpu.VMEM((n, D), BF16), pltpu.VMEM((D, n), BF16), pltpu.VMEM((n, D), F32),
            pltpu.VMEM((n, D), F32), pltpu.VMEM((groups, n, hidden), BF16),
            pltpu.VMEM((groups, n, hidden), BF16),
            pltpu.VMEM(halves, BF16), pltpu.VMEM(halves, BF16), pltpu.VMEM(halves, BF16),
            pltpu.VMEM(halves, BF16), pltpu.VMEM(halves, BF16),
            pltpu.VMEM((2, Z_DEV, depth, hidden), BF16), pltpu.VMEM((n, D), BF16),
            pltpu.SemaphoreType.DMA((18,)), pltpu.SemaphoreType.DMA((18,)),
            pltpu.SemaphoreType.DMA,
        ],
        compiler_params=pltpu.CompilerParams(
            vmem_limit_bytes=VMEM_LIMIT, collective_id=1, has_side_effects=True
        ),
        name="fused_feed_forward",
    )(length, cot, a2, a2t, h1, g1, g2, rows)


def run_fused_backward(x, g0, rows, dh1, gb, gbt, q, v, kt, p, o, a1t, d1, d2, early):
    n = x.shape[0]
    groups, _, _, width = g0.shape
    heads = width // HEAD_DIM
    hidden = d1.shape[-1]
    depth = D // (Z_DEV * Y_DEV)
    step = n // 4

    def by_group(*shape):
        return pl.BlockSpec(
            (1,) + shape, lambda t: (group_order(t % 4),) + (0,) * len(shape)
        )

    p_spec = pl.BlockSpec(
        (1, heads, step, n), lambda t: (group_order(t % 4), 0, t // 4, 0)
    )
    o_spec = pl.BlockSpec(
        (1, n, width), lambda t: (group_order(jnp.minimum(t, 3)), 0, 0)
    )
    copies = 60
    block = (Z_DEV, depth, hidden)
    narrow = (Z_DEV, depth, width)
    return pl.pallas_call(
        fused_backward,
        grid=(4 * groups,),
        in_specs=[
            VMEM_WHOLE, by_group(4, D, width), VMEM_WHOLE, VMEM_WHOLE, VMEM_WHOLE, VMEM_WHOLE,
            by_group(n, width), by_group(n, width), by_group(width, n), p_spec, o_spec,
            VMEM_WHOLE, VMEM_WHOLE, VMEM_WHOLE, VMEM_WHOLE,
        ],
        out_specs=[ANY_WHOLE] + [VMEM_WHOLE] * 4,
        out_shape=[
            shaped(BF16, groups, n, D), shaped(F32, 4, depth, width),
            shaped(F32, depth, hidden), shaped(F32, depth, hidden), shaped(F32, 16, D),
        ],
        scratch_shapes=[
            pltpu.VMEM((groups, n, width), BF16), pltpu.VMEM((groups, 16, n), F32),
            pltpu.VMEM((groups, width, n), F32), pltpu.VMEM((groups, n, width), BF16),
            pltpu.VMEM((groups, n, width), BF16), pltpu.VMEM((groups, n, width), BF16),
            pltpu.VMEM((step, D), F32), pltpu.VMEM((n, D), BF16),
            pltpu.VMEM((groups, 8, width), F32),
            pltpu.VMEM((2,) + block, BF16), pltpu.VMEM((2,) + block, BF16),
            pltpu.VMEM(block, BF16), pltpu.VMEM((3, depth, hidden), BF16),
            pltpu.VMEM(block, BF16), pltpu.VMEM(block, BF16),
            pltpu.VMEM((3, depth, hidden), BF16),
            pltpu.VMEM((2, Z_DEV, Y_DEV, depth, width), BF16),
            pltpu.VMEM((2, Z_DEV, Y_DEV, depth, width), BF16),
            pltpu.VMEM((2, Z_DEV, Y_DEV, depth, width), BF16),
            pltpu.VMEM((2,) + narrow, BF16), pltpu.VMEM(narrow, BF16),
            pltpu.VMEM((3, depth, width), BF16),
            pltpu.VMEM((2, 3, Z_DEV, Y_DEV, depth, width), BF16),
            pltpu.VMEM((2, 3, Z_DEV, Y_DEV, depth, width), BF16),
            pltpu.VMEM((2, 3, Z_DEV, Y_DEV, depth, width), BF16),
            pltpu.VMEM((2, 2) + narrow, BF16),
            pltpu.VMEM((Z_DEV, Y_DEV, depth, width), BF16),
            pltpu.VMEM((3,) + narrow, BF16), pltpu.VMEM((3, 3, depth, width), BF16),
            pltpu.VMEM((4, 16, D), F32), pltpu.VMEM((6, 16, D), F32),
            pltpu.SemaphoreType.DMA((copies,)), pltpu.SemaphoreType.DMA((copies,)),
            pltpu.SemaphoreType.DMA((4,)),
        ],
        compiler_params=pltpu.CompilerParams(
            vmem_limit_bytes=VMEM_LIMIT, collective_id=2, has_side_effects=True
        ),
        name="fused_backward",
    )(x, g0, rows, dh1, gb, gbt, q, v, kt, p, o, a1t, d1, d2, early)


def on_device(
    fused,
    tokens, lengths, tie_map, norm_gains, bias_rows, attention_in, attention_out,
    expand_weight, project_weight, cotangent,
):
    slot_rows = tokens.shape[0] // lengths.shape[0]
    me = lax.axis_index("tensor")
    in_local = lax.dynamic_index_in_dim(attention_in, tie_map[0], 0, keepdims=False)
    out_local = lax.dynamic_index_in_dim(attention_out, tie_map[1], 0, keepdims=False)
    expand_local = lax.dynamic_index_in_dim(expand_weight, tie_map[2], 0, keepdims=False)
    project_local = lax.dynamic_index_in_dim(project_weight, tie_map[3], 0, keepdims=False)
    local0 = jnp.concatenate([in_local, out_local.T[None]], 0)
    row_kinds = jnp.array([0, 0, 0, 1, 2, 3] + [2] * (FF // D), dtype=jnp.int32)
    gain_kinds = jnp.array([0, 2], dtype=jnp.int32)
    gain_pick = norm_gains[tie_map[gain_kinds], jnp.arange(2)]
    bias_pick = bias_rows[tie_map[row_kinds], jnp.arange(row_kinds.shape[0])]
    vectors = jnp.concatenate([gain_pick, bias_pick], 0)
    x = lax.dynamic_slice_in_dim(tokens, me * slot_rows, slot_rows, 0)
    cot = lax.dynamic_slice_in_dim(cotangent, me * slot_rows, slot_rows, 0)
    length = lax.dynamic_slice_in_dim(lengths, me, 1, 0)
    local = (local0, expand_local, project_local.T, vectors)
    run = fused_step if fused else plain_step
    layer_out, tokens_grad, *parts = run(x, cot, length, *local)
    return layer_out, tokens_grad, *placed(tie_map, *parts)


def plain_step(x, cot, length, local0, local1, local2, vectors):
    rows = lax.all_gather(vectors, ("dp", "tensor"), axis=1, tiled=True).astype(F32)
    rows = jnp.concatenate([rows, jnp.zeros((4, D), F32)], 0)

    def gathered(piece, axis):
        piece = lax.all_gather(piece, "dp", axis=axis, tiled=True)
        return lax.all_gather(piece, "tensor", axis=0)

    g0 = gathered(local0, 1)
    g1 = gathered(local1, 0)
    g2 = gathered(local2, 0)
    groups, width = g0.shape[0], g0.shape[-1]
    bqv = rows[3:5].reshape(2, groups, width).transpose(1, 0, 2)
    q, v, kt, p, o, a1t, h1, a2, a2t = run_attention_forward(length, x, g0, rows, bqv)
    out, d1, d2, dh1, gb, gbt, sums = run_feed_forward(length, cot, a2, a2t, h1, g1, g2, rows)
    d0, xg, sums_in, sums_qv = run_attention_backward(
        x, g0, rows, dh1, gb, gbt, q, v, kt, p, o, a1t
    )
    layer_out = lax.all_gather(out, "tensor", axis=0, tiled=True)
    tokens_grad = lax.all_gather(xg, "tensor", axis=0, tiled=True)

    def scattered(piece, axis):
        piece = lax.psum_scatter(piece, "tensor", scatter_dimension=0)
        return lax.psum_scatter(piece, "dp", scatter_dimension=axis, tiled=True).astype(F32)

    part0 = scattered(d0, 1)
    part1 = scattered(d1, 0)
    part2 = scattered(d2, 0)
    qv = sums_qv[:, :2].transpose(1, 0, 2).reshape(2, D)
    sums = jnp.concatenate(
        [sums_in[0:1], sums[1:2], sums_in[1:2], qv, sums[5:12]], 0
    )
    sums = lax.psum_scatter(sums, ("dp", "tensor"), scatter_dimension=1, tiled=True)
    return layer_out, tokens_grad, sums, part0, part1, part2


def fused_step(x, cot, length, local0, local1, local2, vectors):
    kinds, own = vectors.shape
    vec = jnp.pad(vectors.astype(F32).T, ((0, 0), (0, 128 - kinds)))
    g0, g1, g2, rows, q, v, kt, p, o, a1t, h1, a2, a2t = run_fused_forward(
        length, x, local0, local1, local2, vec
    )
    g1 = g1.reshape(g1.shape[0], D, -1)
    g2 = g2.reshape(g2.shape[0], D, -1)
    out, d1, d2, dh1, gb, gbt, early = run_fused_feed_forward(
        length, cot, a2, a2t, h1, g1, g2, rows
    )
    grad, part0, part1, part2, sums = run_fused_backward(
        x, g0, rows, dh1, gb, gbt, q, v, kt, p, o, a1t, d1, d2, early
    )
    first = (lax.axis_index("dp") * 4 + lax.axis_index("tensor")) * own
    sums = lax.dynamic_slice_in_dim(sums[:kinds], first, own, 1)
    return out.reshape(-1, D), grad.reshape(-1, D), sums, part0, part1, part2


def placed(tie_map, sums, part0, part1, part2):
    source = jnp.arange(NSRC, dtype=jnp.int32)

    def place(piece, which):
        pick = (source == tie_map[which]).reshape((NSRC,) + (1,) * piece.ndim)
        return jnp.where(pick, piece[None], 0.0)

    def place_rows(piece, kinds):
        pick = source[:, None] == tie_map[jnp.array(kinds, dtype=jnp.int32)][None, :]
        return jnp.where(pick[:, :, None], piece[None], 0.0)

    return (
        place_rows(sums[:2], [0, 2]),
        place_rows(sums[2:], [0, 0, 0, 1, 2, 3] + [2] * (FF // D)),
        place(part0[:3], 0),
        place(part0[3].T, 1),
        place(part1, 2),
        place(part2.T, 3),
    )


def solution(mesh):
    fused = mesh.shape["dp"] == Z_DEV * Y_DEV and mesh.shape["tensor"] == X_DEV * C_DEV
    return jax.shard_map(
        partial(on_device, fused),
        mesh=mesh,
        in_specs=(
            P("dp", None),
            P("dp"),
            P(),
            P(None, None, ("dp", "tensor")),
            P(None, None, ("dp", "tensor")),
            P(None, None, "dp", "tensor"),
            P(None, "tensor", "dp"),
            P(None, "dp", "tensor"),
            P(None, "tensor", "dp"),
            P("dp", None),
        ),
        out_specs=(
            P("dp", None),
            P("dp", None),
            P(None, None, ("dp", "tensor")),
            P(None, None, ("dp", "tensor")),
            P(None, None, "dp", "tensor"),
            P(None, "tensor", "dp"),
            P(None, "dp", "tensor"),
            P(None, "tensor", "dp"),
        ),
        check_vma=False,
    )
```

```python
import jax
import jax.numpy as jnp
from jax import lax
from jax.experimental import pallas as pl
from jax.experimental.pallas import tpu as pltpu
from jax.sharding import PartitionSpec as P

D = 768
HEAD_DIM = 64
FF = 3072
NSRC = 4
EPS = 1e-05
MASKED = -1e30
F32 = jnp.float32
BF16 = jnp.bfloat16
VMEM_LIMIT = 60 * 1024 * 1024


def dot_nn(a, b):
    return lax.dot_general(a, b, (((1,), (0,)), ((), ())), preferred_element_type=F32)


def dot_nt(a, b):
    return lax.dot_general(a, b, (((1,), (1,)), ((), ())), preferred_element_type=F32)


def norm_parts(v):
    center = jnp.mean(v, -1, keepdims=True)
    centered = v - center
    r = lax.rsqrt(jnp.mean(centered * centered, -1, keepdims=True) + EPS)
    return centered * r, r


def head_mask(shape, h):
    lane = lax.broadcasted_iota(jnp.int32, shape, 1)
    return (lane >= h * HEAD_DIM) & (lane < (h + 1) * HEAD_DIM)


def blocks(total, size):
    return [slice(i * size, (i + 1) * size) for i in range(total // size)]


def attention_forward(
    len_ref, x_ref, g_ref, rows_ref, bqv_ref,
    q_ref, v_ref, kt_ref, p_ref, o_ref, a1t_ref, h1_ref, a2_ref, a2t_ref,
    a1_ref, k_ref, vt_ref, ot_ref, attn_ref,
):
    t = pl.program_id(0)
    n = x_ref.shape[0]
    width = g_ref.shape[-1]
    heads = width // HEAD_DIM
    step = 256
    length = len_ref[0]

    @pl.when(t == 0)
    def _():
        @pl.loop(0, n // step)
        def _(b):
            rows = pl.ds(pl.multiple_of(b * step, step), step)
            xhat, _ = norm_parts(x_ref[rows, :].astype(F32))
            a1 = xhat * rows_ref[0:1, :] + rows_ref[2:3, :]
            a1_ref[rows, :] = a1.astype(BF16)
            a1t_ref[:, rows] = a1.astype(BF16).T
            attn_ref[rows, :] = x_ref[rows, :].astype(F32) + rows_ref[5:6, :]

    @pl.loop(0, n // step)
    def _(b):
        rows = pl.ds(pl.multiple_of(b * step, step), step)
        a1 = a1_ref[rows, :]
        q = (dot_nn(a1, g_ref[0, 0]) + bqv_ref[0, 0:1, :]).astype(BF16)
        q_ref[0, rows, :] = q * jnp.asarray(HEAD_DIM ** -0.5, BF16)
        k = dot_nn(a1, g_ref[0, 1]).astype(BF16)
        k_ref[rows, :] = k
        kt_ref[0, :, rows] = k.T
        v = (dot_nn(a1, g_ref[0, 2]) + bqv_ref[0, 1:2, :]).astype(BF16)
        v_ref[0, rows, :] = v
        vt_ref[:, rows] = v.T

    for h in range(heads):
        k = k_ref[...]
        k = jnp.where(head_mask(k.shape, h), k, jnp.zeros_like(k))
        for b in range(n // step):
            first, last = b * step, (b + 1) * step
            q = q_ref[0, first:last, :]
            key = lax.broadcasted_iota(jnp.int32, (last, step), 0)
            query = lax.broadcasted_iota(jnp.int32, (step, step), 1) + first
            s = dot_nt(k[:last], q)
            near = jnp.where(
                (key[first:] <= query) & (key[first:] < length), s[first:], MASKED
            )
            if b:
                far = jnp.where(key[:first] < length, s[:first], MASKED)
                top = jnp.maximum(
                    jnp.max(far, 0, keepdims=True), jnp.max(near, 0, keepdims=True)
                )
                e_far = jnp.exp(far - top)
                e_near = jnp.exp(near - top)
                total = jnp.sum(e_far, 0, keepdims=True) + jnp.sum(e_near, 0, keepdims=True)
                scale = 1.0 / total
                p_ref[0, h, :first, first:last] = (e_far * scale).astype(BF16)
            else:
                top = jnp.max(near, 0, keepdims=True)
                e_near = jnp.exp(near - top)
                scale = 1.0 / jnp.sum(e_near, 0, keepdims=True)
            p_ref[0, h, first:last, first:last] = (e_near * scale).astype(BF16)
            ot_ref[h * HEAD_DIM : (h + 1) * HEAD_DIM, first:last] = dot_nn(
                vt_ref[h * HEAD_DIM : (h + 1) * HEAD_DIM, :last],
                p_ref[0, h, :last, first:last],
            ).astype(BF16)

    @pl.loop(0, n // step)
    def _(b):
        rows = pl.ds(pl.multiple_of(b * step, step), step)
        o = ot_ref[:, rows].T
        o_ref[0, rows, :] = o
        attn_ref[rows, :] += dot_nt(o, g_ref[0, 3])

    @pl.when(t == pl.num_programs(0) - 1)
    def _():
        @pl.loop(0, n // step)
        def _(b):
            rows = pl.ds(pl.multiple_of(b * step, step), step)
            h1 = attn_ref[rows, :]
            h1_ref[rows, :] = h1
            xhat, _ = norm_parts(h1)
            a2 = (xhat * rows_ref[1:2, :] + rows_ref[6:7, :]).astype(BF16)
            a2_ref[rows, :] = a2
            a2t_ref[:, rows] = a2.T


SQRT_2_PI = 0.7978845608028654


def feed_forward_both(
    len_ref, c_ref, a2_ref, a2t_ref, h1_ref, w1_ref, w2_ref, rows_ref,
    out_ref, d1_ref, d2_ref, dh1_ref, gb_ref, gbt_ref, sums_ref,
    gf_ref, gft_ref, feed_ref, da2_ref, h_ref, df_ref,
):
    t = pl.program_id(0)
    n = c_ref.shape[0]
    step = 256
    length = len_ref[0]

    @pl.when(t == 0)
    def _():
        sums_ref[...] = jnp.zeros_like(sums_ref)

        @pl.loop(0, n // step)
        def _(b):
            rows = pl.ds(pl.multiple_of(b * step, step), step)
            place = b * step + lax.broadcasted_iota(jnp.int32, (step, 1), 0)
            live = (place < length).astype(F32)
            g = (c_ref[rows, :].astype(F32) * live).astype(BF16)
            gf_ref[rows, :] = g
            gft_ref[:, rows] = g.T
            sums_ref[7:8, :] += jnp.sum(g.astype(F32), 0, keepdims=True)

    bias = rows_ref[pl.ds(8 + t, 1), :]

    @pl.loop(0, n // step)
    def _(b):
        rows = pl.ds(pl.multiple_of(b * step, step), step)
        f = dot_nn(a2_ref[rows, :], w1_ref[0]) + bias
        dh = dot_nn(gf_ref[rows, :], w2_ref[0])
        f2 = f * f
        th = jnp.tanh(f * (SQRT_2_PI + (SQRT_2_PI * 0.044715) * f2))
        half = 0.5 + 0.5 * th
        h = (f * half).astype(BF16)
        slope = half + f * (0.5 - 0.5 * th * th) * (
            SQRT_2_PI + (3 * SQRT_2_PI * 0.044715) * f2
        )
        df = (dh * slope).astype(BF16)
        h_ref[rows, :] = h
        df_ref[rows, :] = df
        sums_ref[pl.ds(8 + t, 1), :] += jnp.sum(df.astype(F32), 0, keepdims=True)
        feed = dot_nt(h, w2_ref[0])
        da2 = dot_nt(df, w1_ref[0])

        @pl.when(t == 0)
        def _():
            feed_ref[rows, :] = feed
            da2_ref[rows, :] = da2

        @pl.when(t > 0)
        def _():
            feed_ref[rows, :] += feed
            da2_ref[rows, :] += da2

    @pl.loop(0, D // step)
    def _(b):
        rows = pl.ds(pl.multiple_of(b * step, step), step)
        d1_ref[0, rows, :] = dot_nn(a2t_ref[rows, :], df_ref[...]).astype(BF16)
        d2_ref[0, rows, :] = dot_nn(gft_ref[rows, :], h_ref[...]).astype(BF16)

    @pl.when(t == pl.num_programs(0) - 1)
    def _():
        @pl.loop(0, n // step)
        def _(b):
            rows = pl.ds(pl.multiple_of(b * step, step), step)
            place = b * step + lax.broadcasted_iota(jnp.int32, (step, 1), 0)
            live = (place < length).astype(F32)
            h1 = h1_ref[rows, :]
            out_ref[rows, :] = (live * (h1 + (feed_ref[rows, :] + rows_ref[7:8, :]))).astype(BF16)
            xhat, r = norm_parts(h1)
            da2 = da2_ref[rows, :]
            sums_ref[1:2, :] += jnp.sum(da2 * xhat, 0, keepdims=True)
            sums_ref[6:7, :] += jnp.sum(da2, 0, keepdims=True)
            dg = da2 * rows_ref[1:2, :]
            dv = r * (
                dg
                - jnp.mean(dg, -1, keepdims=True)
                - xhat * jnp.mean(dg * xhat, -1, keepdims=True)
            )
            dh1 = live * c_ref[rows, :].astype(F32) + dv
            dh1_ref[rows, :] = dh1
            gb = dh1.astype(BF16)
            gb_ref[rows, :] = gb
            gbt_ref[:, rows] = gb.T
            sums_ref[5:6, :] += jnp.sum(gb.astype(F32), 0, keepdims=True)


def attention_backward(
    x_ref, g_ref, rows_ref, dh1_ref, gb_ref, gbt_ref, q_ref, v_ref, kt_ref, p_ref,
    o_ref, a1t_ref,
    d0_ref, xg_ref, sums_ref, bqv_ref,
    do_ref, delta_ref, dqt_ref, dq_ref, dk_ref, dv_ref, da1_ref,
):
    t = pl.program_id(0)
    n = x_ref.shape[0]
    width = g_ref.shape[-1]
    heads = width // HEAD_DIM
    step = 256
    pick = (
        lax.broadcasted_iota(jnp.int32, (16, width), 1) // HEAD_DIM
        == lax.broadcasted_iota(jnp.int32, (16, width), 0)
    ).astype(BF16)

    @pl.loop(0, n // step)
    def _(b):
        rows = pl.ds(pl.multiple_of(b * step, step), step)
        do = dot_nn(gb_ref[rows, :], g_ref[0, 3]).astype(BF16)
        do_ref[rows, :] = do
        prod = do.astype(F32) * o_ref[0, rows, :].astype(F32)
        high = prod.astype(BF16)
        low = (prod - high.astype(F32)).astype(BF16)
        delta_ref[:, rows] = dot_nt(pick, high) + dot_nt(pick, low)

    dqt_ref[...] = jnp.zeros_like(dqt_ref)
    for b in range(n // step):
        first, last = b * step, (b + 1) * step
        do = do_ref[first:, :]
        q = q_ref[0, first:, :]
        v = v_ref[0, first:last, :]
        dk, dv = None, None
        for h in range(heads):
            mine = head_mask((1, width), h)
            zero = jnp.zeros((), BF16)
            p = p_ref[0, h, first:last, first:]
            dp = dot_nt(jnp.where(mine, v, zero), do)
            ds = (p.astype(F32) * (dp - delta_ref[h : h + 1, first:])).astype(BF16)
            part = dot_nn(p, jnp.where(mine, do, zero))
            dv = part if dv is None else dv + part
            part = dot_nn(ds, jnp.where(mine, q, zero))
            dk = part if dk is None else dk + part
            head = slice(h * HEAD_DIM, (h + 1) * HEAD_DIM)
            dqt_ref[head, first:] += dot_nn(kt_ref[0, head, first:last], ds)
        dk_ref[first:last, :] = dk.astype(BF16)
        dv_ref[first:last, :] = dv.astype(BF16)

    @pl.when(t == 0)
    def _():
        da1_ref[...] = jnp.zeros_like(da1_ref)

    bqv_ref[...] = jnp.zeros_like(bqv_ref)

    @pl.loop(0, n // step)
    def _(b):
        rows = pl.ds(pl.multiple_of(b * step, step), step)
        dq = (dqt_ref[:, rows] * HEAD_DIM ** -0.5).astype(BF16).T
        dk = dk_ref[rows, :]
        dv = dv_ref[rows, :]
        dq_ref[rows, :] = dq
        bqv_ref[0, 0:1, :] += jnp.sum(dq.astype(F32), 0, keepdims=True)
        bqv_ref[0, 1:2, :] += jnp.sum(dv.astype(F32), 0, keepdims=True)
        da1_ref[rows, :] += (
            dot_nt(dq, g_ref[0, 0]) + dot_nt(dk, g_ref[0, 1]) + dot_nt(dv, g_ref[0, 2])
        )

    @pl.loop(0, D // step)
    def _(b):
        rows = pl.ds(pl.multiple_of(b * step, step), step)
        a1t = a1t_ref[rows, :]
        d0_ref[0, 0, rows, :] = dot_nn(a1t, dq_ref[...]).astype(BF16)
        d0_ref[0, 1, rows, :] = dot_nn(a1t, dk_ref[...]).astype(BF16)
        d0_ref[0, 2, rows, :] = dot_nn(a1t, dv_ref[...]).astype(BF16)
        d0_ref[0, 3, rows, :] = dot_nn(gbt_ref[rows, :], o_ref[0]).astype(BF16)

    @pl.when(t == pl.num_programs(0) - 1)
    def _():
        sums_ref[...] = jnp.zeros_like(sums_ref)

        @pl.loop(0, n // step)
        def _(b):
            rows = pl.ds(pl.multiple_of(b * step, step), step)
            xhat, r = norm_parts(x_ref[rows, :].astype(F32))
            da1 = da1_ref[rows, :]
            sums_ref[0:1, :] += jnp.sum(da1 * xhat, 0, keepdims=True)
            sums_ref[1:2, :] += jnp.sum(da1, 0, keepdims=True)
            dg = da1 * rows_ref[0:1, :]
            dv = r * (
                dg
                - jnp.mean(dg, -1, keepdims=True)
                - xhat * jnp.mean(dg * xhat, -1, keepdims=True)
            )
            xg_ref[rows, :] = (dh1_ref[rows, :] + dv).astype(BF16)


def whole(*shape):
    return pl.BlockSpec(shape, lambda t: (0,) * len(shape))


def group(*shape):
    return pl.BlockSpec((1,) + shape, lambda t: (t,) + (0,) * len(shape))


def shaped(dtype, *shape):
    return jax.ShapeDtypeStruct(shape, dtype)


SMEM_WHOLE = pl.BlockSpec(memory_space=pltpu.SMEM)


def run_attention_forward(length, x, g0, rows, bqv):
    n = x.shape[0]
    groups, _, _, width = g0.shape
    heads = width // HEAD_DIM
    return pl.pallas_call(
        attention_forward,
        grid=(groups,),
        in_specs=[SMEM_WHOLE, whole(n, D), group(4, D, width), whole(16, D), group(2, width)],
        out_specs=[
            group(n, width), group(n, width), group(width, n), group(heads, n, n),
            group(n, width), whole(D, n), whole(n, D), whole(n, D), whole(D, n),
        ],
        out_shape=[
            shaped(BF16, groups, n, width), shaped(BF16, groups, n, width),
            shaped(BF16, groups, width, n), shaped(BF16, groups, heads, n, n),
            shaped(BF16, groups, n, width), shaped(BF16, D, n), shaped(F32, n, D),
            shaped(BF16, n, D), shaped(BF16, D, n),
        ],
        scratch_shapes=[
            pltpu.VMEM((n, D), BF16), pltpu.VMEM((n, width), BF16),
            pltpu.VMEM((width, n), BF16), pltpu.VMEM((width, n), BF16),
            pltpu.VMEM((n, D), F32),
        ],
        compiler_params=pltpu.CompilerParams(vmem_limit_bytes=VMEM_LIMIT),
        name="attention_forward",
    )(length, x, g0, rows, bqv)


def run_feed_forward(length, cot, a2, a2t, h1, g1, g2, rows):
    n = cot.shape[0]
    groups, _, width = g1.shape
    return pl.pallas_call(
        feed_forward_both,
        grid=(groups,),
        in_specs=[
            SMEM_WHOLE, whole(n, D), whole(n, D), whole(D, n), whole(n, D),
            group(D, width), group(D, width), whole(16, D),
        ],
        out_specs=[
            whole(n, D), group(D, width), group(D, width), whole(n, D), whole(n, D),
            whole(D, n), whole(16, D),
        ],
        out_shape=[
            shaped(BF16, n, D), shaped(BF16, groups, D, width), shaped(BF16, groups, D, width),
            shaped(F32, n, D), shaped(BF16, n, D), shaped(BF16, D, n), shaped(F32, 16, D),
        ],
        scratch_shapes=[
            pltpu.VMEM((n, D), BF16), pltpu.VMEM((D, n), BF16), pltpu.VMEM((n, D), F32),
            pltpu.VMEM((n, D), F32), pltpu.VMEM((n, width), BF16), pltpu.VMEM((n, width), BF16),
        ],
        compiler_params=pltpu.CompilerParams(vmem_limit_bytes=VMEM_LIMIT),
        name="feed_forward_both",
    )(length, cot, a2, a2t, h1, g1, g2, rows)


def run_attention_backward(x, g0, rows, dh1, gb, gbt, q, v, kt, p, o, a1t):
    n = x.shape[0]
    groups, _, _, width = g0.shape
    heads = width // HEAD_DIM
    return pl.pallas_call(
        attention_backward,
        grid=(groups,),
        in_specs=[
            whole(n, D), group(4, D, width), whole(16, D), whole(n, D), whole(n, D),
            whole(D, n), group(n, width), group(n, width), group(width, n),
            group(heads, n, n), group(n, width), whole(D, n),
        ],
        out_specs=[group(4, D, width), whole(n, D), whole(8, D), group(8, width)],
        out_shape=[
            shaped(BF16, groups, 4, D, width), shaped(BF16, n, D), shaped(F32, 8, D),
            shaped(F32, groups, 8, width),
        ],
        scratch_shapes=[
            pltpu.VMEM((n, width), BF16), pltpu.VMEM((16, n), F32), pltpu.VMEM((width, n), F32),
            pltpu.VMEM((n, width), BF16), pltpu.VMEM((n, width), BF16),
            pltpu.VMEM((n, width), BF16), pltpu.VMEM((n, D), F32),
        ],
        compiler_params=pltpu.CompilerParams(vmem_limit_bytes=VMEM_LIMIT),
        name="attention_backward",
    )(x, g0, rows, dh1, gb, gbt, q, v, kt, p, o, a1t)


Z_DEV, Y_DEV, X_DEV, C_DEV = 4, 2, 2, 2


class Place:
    def __init__(self):
        dp, self.t = lax.axis_index("dp"), lax.axis_index("tensor")
        self.dp = dp
        self.z, self.y = dp // 2, dp % 2
        self.x, self.c = self.t // 2, self.t % 2
        self.other_y = 1 - self.y
        self.zs = [
            self.z,
            self.z + 1 - 2 * (self.z % 2),
            self.z + 2 - 4 * (self.z // 2),
            3 - self.z,
        ]
        self.ts = [
            self.t,
            self.t + 1 - 2 * (self.t % 2),
            self.t + 2 - 4 * (self.t // 2),
            3 - self.t,
        ]
        self.to_z = [dict(dp=z * 2 + self.y) for z in self.zs]
        self.to_y = dict(dp=self.z * 2 + self.other_y)
        self.to_x = dict(tensor=self.ts[2])
        self.to_core = dict(tensor=self.ts[1])

    def group(self, k):
        return lax.select(
            k == 0, self.ts[0],
            lax.select(k == 1, self.ts[1], lax.select(k == 2, self.ts[2], self.ts[3])),
        )

    def greet(self):
        barrier = pltpu.get_barrier_semaphore()
        others = self.to_z[1:] + [self.to_y, self.to_x, self.to_core]
        for device in others:
            pl.semaphore_signal(
                barrier, inc=1, device_id=device, device_id_type=pl.DeviceIdType.MESH
            )
        pl.semaphore_wait(barrier, len(others))


class Links:
    def __init__(self, send_sem, recv_sem):
        self.send_sem, self.recv_sem = send_sem, recv_sem
        self.copies = []

    def add(self, device, src, dst):
        number = len(self.copies)
        copy = pltpu.make_async_remote_copy(
            src_ref=src,
            dst_ref=dst,
            send_sem=self.send_sem.at[number],
            recv_sem=self.recv_sem.at[number],
            device_id=device,
            device_id_type=pl.DeviceIdType.MESH,
        )
        self.copies.append(copy)
        return copy

    def sent(self, *apart):
        for copy in self.copies:
            if all(copy is not other for other in apart):
                copy.wait_send()


def flat(copies):
    for item in copies:
        if isinstance(item, list):
            yield from flat(item)
        else:
            yield item


def start(*copies):
    for copy in flat(copies):
        copy.start()


def recv(*copies):
    for copy in flat(copies):
        copy.wait_recv()


class Gather:
    def __init__(self, links, place, own, full, x_first, single=True):
        every = slice(None)
        y, other = place.y, place.other_y

        def same(device, k, yy, to):
            return links.add(device, full(k, every, yy), full(to, every, yy))

        if x_first:
            self.first = [links.add(place.to_x, own, full(2, place.z, y))]
        self.z = [
            links.add(place.to_z[k], own, full(0, place.z, y)) for k in range(1, 4)
        ]
        if x_first:
            far = full(2, place.z, y)
            self.far = [links.add(place.to_z[k], far, far) for k in range(1, 4)]
            self.second = [same(place.to_y, 0, y, 0), same(place.to_y, 2, y, 2)]
            blocks = [(0, y), (2, y), (0, other), (2, other)]
        else:
            if single:
                self.first = [same(place.to_y, 0, y, 0)]
            else:
                self.first = [links.add(place.to_y, own, full(0, place.z, y))]
                for k in range(1, 4):
                    block = full(0, place.zs[k], y)
                    self.first.append(links.add(place.to_y, block, block))
            self.second = [same(place.to_x, 0, y, 2), same(place.to_x, 0, other, 2)]
            blocks = [(0, y), (0, other), (2, y), (2, other)]
        self.core = [same(place.to_core, k, yy, k + 1) for k, yy in blocks]


def fused_forward(
    tie_ref, len_ref, tokens_ref, gains_ref, bias_ref, in_ref, out_ref, expand_ref,
    project_ref,
    gq_ref, gw_ref, w1_ref, w2_ref, rows_ref,
    q_ref, v_ref, kt_ref, p_ref, o_ref, a1t_ref, h1_ref, a2_ref, a2t_ref,
    own0_ref, ownw_ref, own1_ref, own2_ref, square_ref, vec_ref,
    all0_ref, allw_ref, vecs_ref, bqv_ref, x_ref, a1_ref, k_ref, vt_ref, ot_ref, attn_ref,
    send_sem, recv_sem, local_sem,
):
    t = pl.program_id(0)
    n, _ = x_ref.shape
    width = allw_ref.shape[-1]
    heads = width // HEAD_DIM
    step = 256
    place = Place()
    length = len_ref[place.t]
    links = Links(send_sem, recv_sem)
    z, y, x, c = place.z, place.y, place.x, place.c
    vec_z = [
        links.add(place.to_z[k], vec_ref, vecs_ref.at[z, y, x, c]) for k in range(1, 4)
    ]
    vec_y = links.add(place.to_y, vecs_ref.at[:, y, x, c], vecs_ref.at[:, y, x, c])
    vec_x = links.add(place.to_x, vecs_ref.at[:, :, x, c], vecs_ref.at[:, :, x, c])
    vec_core = links.add(place.to_core, vecs_ref.at[:, :, :, c], vecs_ref.at[:, :, :, c])
    seg0 = Gather(
        links, place, own0_ref, lambda k, z, y: all0_ref.at[k, z, y], False, False
    )
    segw = Gather(links, place, ownw_ref, lambda k, z, y: allw_ref.at[k, z, y], False)
    seg1 = Gather(links, place, own1_ref, lambda k, z, y: w1_ref.at[k, z, y], False)
    seg2 = Gather(links, place, own2_ref, lambda k, z, y: w2_ref.at[k, z, y], True)
    keep1 = pltpu.make_async_copy(own1_ref, w1_ref.at[0, z, y], local_sem.at[0])
    keep2 = pltpu.make_async_copy(own2_ref, w2_ref.at[0, z, y], local_sem.at[1])
    fetch = pltpu.make_async_copy(tokens_ref.at[place.t], x_ref, local_sem.at[2])

    def pass_on(seg, stage):
        if stage == 0:
            recv(seg.z)
            start(seg.first, seg.second[0], seg.core[0])
        elif stage == 1:
            recv(seg.first)
            start(seg.second[1], seg.core[1])
        else:
            recv(seg.second[stage - 2])
            start(seg.core[stage])

    @pl.when(t == 0)
    def _():
        s0, s1, s2, s3 = tie_ref[0], tie_ref[1], tie_ref[2], tie_ref[3]
        fetch.start()
        square_ref[...] = jnp.zeros_like(square_ref)
        gain = gains_ref.shape[-1]
        square_ref[0:1, :gain] = gains_ref[s0].astype(F32)[0:1]
        square_ref[1:2, :gain] = gains_ref[s2].astype(F32)[1:2]
        square_ref[2:5, :gain] = bias_ref[s0].astype(F32)[0:3]
        square_ref[5:6, :gain] = bias_ref[s1].astype(F32)[3:4]
        square_ref[6:7, :gain] = bias_ref[s2].astype(F32)[4:5]
        square_ref[7:8, :gain] = bias_ref[s3].astype(F32)[5:6]
        square_ref[8:12, :gain] = bias_ref[s2].astype(F32)[6:10]
        vec_ref[...] = square_ref[...].T[:gain]
        for j in range(3):
            own0_ref[:, j * width : (j + 1) * width] = in_ref[s0, j]
        place.greet()
        start(vec_z, seg0.z[1], seg0.z[2], seg0.z[0], seg0.first[0])
        vecs_ref[z, y, x, c] = vec_ref[...]
        all0_ref[0, z, y] = own0_ref[...]
        ownw_ref[...] = out_ref[s1].T
        allw_ref[0, z, y] = ownw_ref[...]
        own1_ref[...] = expand_ref[s2]
        own2_ref[...] = project_ref[s3].T
        keep1.start()
        keep2.start()
        recv(vec_z)
        start(vec_y)
        recv(seg0.z[0])
        start(seg0.first[1])
        recv(vec_y)
        start(vec_x)
        recv(vec_x)
        start(vec_core)
        recv(seg0.z[1])
        start(seg0.first[2])
        start(segw.z, seg2.first, seg1.z, seg2.z)
        recv(vec_core)
        vecs = vecs_ref[...].reshape(D, vecs_ref.shape[-1]).T[:16]
        rows_ref[...] = vecs
        for k in range(4):
            part = slice(k * width, (k + 1) * width)
            bqv_ref[k, 0:1, :width] = vecs[3:4, part]
            bqv_ref[k, 0:1, width : 2 * width] = jnp.zeros((1, width), F32)
            bqv_ref[k, 0:1, 2 * width :] = vecs[4:5, part]
        fetch.wait()

        @pl.loop(0, n // step)
        def _(b):
            rows = pl.ds(pl.multiple_of(b * step, step), step)
            wide = x_ref[rows, :].astype(F32)
            xhat, _ = norm_parts(wide)
            a1 = (xhat * rows_ref[0:1, :] + rows_ref[2:3, :]).astype(BF16)
            a1_ref[rows, :] = a1
            a1t_ref[:, rows] = a1.T
            attn_ref[rows, :] = wide + rows_ref[5:6, :]

        recv(seg0.z[2])
        start(seg0.first[3], seg0.second[0], seg0.core[0])
        recv(seg0.first)
        start(seg0.second[1], seg0.core[1])
        keep1.wait()
        keep2.wait()
        pass_on(segw, 0)

    @pl.when(t == 1)
    def _():
        recv(seg0.core[0], seg0.core[1])

    @pl.when(t == 2)
    def _():
        recv(seg2.z)
        start(seg2.second[0], seg2.core[0])
        pass_on(segw, 3)

    @pl.when(t == 3)
    def _():
        recv(seg0.core[2], seg0.core[3])
        pass_on(seg1, 2)
        recv(seg2.far)
        start(seg2.second[1], seg2.core[1])
        pass_on(seg2, 2)

    gq_ref[0] = all0_ref[t].reshape(gq_ref.shape[1:])
    mine = place.group(t)
    qkv = dot_nn(a1_ref[...], gq_ref[0]) + bqv_ref[mine, 0:1, :]
    q = qkv[:, :width].astype(BF16)
    k = qkv[:, width : 2 * width].astype(BF16)
    v = qkv[:, 2 * width :].astype(BF16)
    q_ref[0] = q * jnp.asarray(HEAD_DIM ** -0.5, BF16)
    k_ref[...] = k
    kt_ref[0] = k.T
    v_ref[0] = v
    vt_ref[...] = v.T

    units = [(h, b) for h in range(heads) for b in range(n // step)]

    def scores(h, b):
        first, last = b * step, (b + 1) * step
        k = k_ref[:last, :]
        k = jnp.where(head_mask((1, width), h), k, jnp.zeros((), BF16))
        return dot_nt(k, q_ref[0, first:last, :])

    def attend(h, b, s):
        first, last = b * step, (b + 1) * step
        key = lax.broadcasted_iota(jnp.int32, (last, step), 0)
        query = lax.broadcasted_iota(jnp.int32, (step, step), 1) + first
        near = jnp.where((key[first:] <= query) & (key[first:] < length), s[first:], MASKED)
        head = slice(h * HEAD_DIM, (h + 1) * HEAD_DIM)
        if b:
            far = jnp.where(key[:first] < length, s[:first], MASKED)
            top = jnp.maximum(jnp.max(far, 0, keepdims=True), jnp.max(near, 0, keepdims=True))
            e_far = jnp.exp(far - top)
            e_near = jnp.exp(near - top)
            total = jnp.sum(e_far, 0, keepdims=True) + jnp.sum(e_near, 0, keepdims=True)
            scale = 1.0 / total
            p_far = (e_far * scale).astype(BF16)
            p_near = (e_near * scale).astype(BF16)
            p_ref[0, h, :first, first:last] = p_far
            o = dot_nn(vt_ref[head, :first], p_far) + dot_nn(vt_ref[head, first:last], p_near)
        else:
            top = jnp.max(near, 0, keepdims=True)
            e_near = jnp.exp(near - top)
            p_near = (e_near * (1.0 / jnp.sum(e_near, 0, keepdims=True))).astype(BF16)
            o = dot_nn(vt_ref[head, :last], p_near)
        p_ref[0, h, first:last, first:last] = p_near
        ot_ref[head, first:last] = o.astype(BF16)

    s = scores(*units[0])
    for i, unit in enumerate(units):
        ahead = scores(*units[i + 1]) if i + 1 < len(units) else None
        attend(*unit, s)
        s = ahead

    @pl.when(t == 0)
    def _():
        pass_on(seg0, 2)
        pass_on(segw, 1)
        pass_on(seg1, 0)

    @pl.when(t == 1)
    def _():
        pass_on(seg0, 3)
        recv(seg2.first)
        start(seg2.far)
        pass_on(seg1, 1)
        recv(segw.core[0], segw.core[1])

    @pl.when(t == 2)
    def _():
        pass_on(segw, 2)

    @pl.when(t == 3)
    def _():
        recv(segw.core[2], segw.core[3])

    gw_ref[0] = allw_ref[t].reshape(gw_ref.shape[1:])
    o = ot_ref[...].T
    o_ref[0] = o
    attn_ref[...] += dot_nt(o, gw_ref[0])

    @pl.when(t == 3)
    def _():
        pass_on(seg1, 3)

        @pl.loop(0, n // step)
        def _(b):
            rows = pl.ds(pl.multiple_of(b * step, step), step)
            h1 = attn_ref[rows, :]
            h1_ref[rows, :] = h1
            xhat, _ = norm_parts(h1)
            a2 = (xhat * rows_ref[1:2, :] + rows_ref[6:7, :]).astype(BF16)
            a2_ref[rows, :] = a2
            a2t_ref[:, rows] = a2.T

        pass_on(seg2, 3)
        recv(seg1.core, seg2.core)
        links.sent()


N_GATHER = 6 + 13 + 10 + 10 + 13
VMEM_WHOLE = pl.BlockSpec(memory_space=pltpu.VMEM)
ANY_WHOLE = pl.BlockSpec(memory_space=pl.ANY)


def run_fused_forward(tie, lengths, tokens, gains, biases, w_in, w_out, w_expand, w_project):
    groups, n, _ = tokens.shape
    depth, width = w_in.shape[-2:]
    heads = width // HEAD_DIM
    hidden = w_expand.shape[-1]
    own = gains.shape[-1]
    return pl.pallas_call(
        fused_forward,
        grid=(groups,),
        in_specs=[SMEM_WHOLE, SMEM_WHOLE, ANY_WHOLE] + [VMEM_WHOLE] * 6,
        out_specs=[
            group(D, 3 * width), group(D, width), ANY_WHOLE, ANY_WHOLE, VMEM_WHOLE,
            group(n, width), group(n, width), group(width, n), group(heads, n, n),
            group(n, width), VMEM_WHOLE, VMEM_WHOLE, VMEM_WHOLE, VMEM_WHOLE,
        ],
        out_shape=[
            shaped(BF16, groups, D, 3 * width), shaped(BF16, groups, D, width),
            shaped(BF16, groups, Z_DEV, Y_DEV, depth, hidden),
            shaped(BF16, groups, Z_DEV, Y_DEV, depth, hidden),
            shaped(F32, 16, D),
            shaped(BF16, groups, n, width), shaped(BF16, groups, n, width),
            shaped(BF16, groups, width, n), shaped(BF16, groups, heads, n, n),
            shaped(BF16, groups, n, width), shaped(BF16, D, n), shaped(F32, n, D),
            shaped(BF16, n, D), shaped(BF16, D, n),
        ],
        scratch_shapes=[
            pltpu.VMEM((depth, 3 * width), BF16), pltpu.VMEM((depth, width), BF16),
            pltpu.VMEM((depth, hidden), BF16), pltpu.VMEM((depth, hidden), BF16),
            pltpu.VMEM((128, 128), F32), pltpu.VMEM((own, 128), F32),
            pltpu.VMEM((groups, Z_DEV, Y_DEV, depth, 3 * width), BF16),
            pltpu.VMEM((groups, Z_DEV, Y_DEV, depth, width), BF16),
            pltpu.VMEM((Z_DEV, Y_DEV, X_DEV, C_DEV, own, 128), F32),
            pltpu.VMEM((groups, 8, 3 * width), F32),
            pltpu.VMEM((n, D), BF16), pltpu.VMEM((n, D), BF16), pltpu.VMEM((n, width), BF16),
            pltpu.VMEM((width, n), BF16), pltpu.VMEM((width, n), BF16),
            pltpu.VMEM((n, D), F32),
            pltpu.SemaphoreType.DMA((N_GATHER,)), pltpu.SemaphoreType.DMA((N_GATHER,)),
            pltpu.SemaphoreType.DMA((3,)),
        ],
        compiler_params=pltpu.CompilerParams(
            vmem_limit_bytes=VMEM_LIMIT, collective_id=0, has_side_effects=True
        ),
        name="fused_forward",
    )(tie, lengths, tokens, gains, biases, w_in, w_out, w_expand, w_project)


def group_order(i):
    return (1 + 2 * i) % 4 - i // 2


def fused_feed_forward(
    len_ref, cot_ref, a2_ref, a2t_ref, h1_ref, w1_ref, w2_ref, rows_ref,
    out_ref, d1_ref, d2_ref, dh1_ref, gb_ref, gbt_ref, sums_ref,
    gf_ref, gft_ref, feed_ref, h_ref, slope_ref,
    land1_ref, stage2_ref, land2_ref, work2_ref, cross2_ref, own_ref, c_ref,
    send_sem, recv_sem, local_sem,
):
    t = pl.program_id(0)
    n = c_ref.shape[0]
    da2_ref, stage1_ref = feed_ref, stage2_ref
    step = 256
    big = 512
    depth = stage2_ref.shape[-2]
    place = Place()
    length = len_ref[place.t]
    links = Links(send_sem, recv_sem)
    y, other = place.y, place.other_y
    quarter = n // 4
    core2 = [links.add(place.to_core, stage2_ref.at[i], land2_ref.at[i]) for i in range(2)]
    core1 = [links.add(place.to_core, stage1_ref.at[i], land1_ref.at[i]) for i in range(2)]
    cross2 = [
        links.add(place.to_y, work2_ref.at[i, :, other], cross2_ref.at[i]) for i in range(2)
    ]
    out_x, out_core, out_far = [], [], []
    for i in range(4):
        rows = pl.ds(i * quarter, quarter)
        mine_there = out_ref.at[place.t, rows]
        far = out_ref.at[place.ts[2], rows]
        out_x.append(links.add(place.to_x, own_ref.at[rows], mine_there))
        out_core.append(links.add(place.to_core, own_ref.at[rows], mine_there))
        out_far.append(links.add(place.to_core, far, far))
    keep = pltpu.make_async_copy(own_ref, out_ref.at[place.t], local_sem.at[0])
    fetch = pltpu.make_async_copy(cot_ref.at[place.t], c_ref, local_sem.at[1])
    k = group_order(t % 4)
    mine = place.group(k)

    def weight_grad(left_ref, right):
        value = dot_nn(left_ref[...], right)
        return value.reshape(Z_DEV, Y_DEV, depth, value.shape[-1])

    @pl.when(t == 0)
    def _():
        fetch.start()
        place.greet()
        sums_ref[...] = jnp.zeros_like(sums_ref)
        fetch.wait()

        @pl.loop(0, n // step)
        def _(b):
            rows = pl.ds(pl.multiple_of(b * step, step), step)
            at = b * step + lax.broadcasted_iota(jnp.int32, (step, 1), 0)
            live = (at < length).astype(F32)
            g = (c_ref[rows, :].astype(F32) * live).astype(BF16)
            gf_ref[rows, :] = g
            gft_ref[:, rows] = g.T
            sums_ref[7:8, :] += jnp.sum(g.astype(F32), 0, keepdims=True)

    @pl.when(t < 4)
    def _():
        bias = rows_ref[pl.ds(8 + mine, 1), :]

        @pl.loop(0, n // big)
        def _(b):
            rows = pl.ds(pl.multiple_of(b * big, big), big)
            f = dot_nn(a2_ref[rows, :], w1_ref[0]) + bias
            f2 = f * f
            th = jnp.tanh(f * (SQRT_2_PI + (SQRT_2_PI * 0.044715) * f2))
            half = 0.5 + 0.5 * th
            h = (f * half).astype(BF16)
            slope = half + f * (0.5 - 0.5 * th * th) * (
                SQRT_2_PI + (3 * SQRT_2_PI * 0.044715) * f2
            )
            h_ref[k, rows, :] = h
            slope_ref[k, rows, :] = slope.astype(BF16)
            feed = dot_nt(h, w2_ref[0])

            @pl.when(t == 0)
            def _():
                feed_ref[rows, :] = feed

            @pl.when(t > 0)
            def _():
                feed_ref[rows, :] += feed

    @pl.when(t < 2)
    def _():
        stage2_ref[t] = weight_grad(gft_ref, h_ref[k]).astype(BF16)
        for i in range(2):
            @pl.when(t == i)
            def _():
                start(core2[i])

    @pl.when(t == 3)
    def _():
        @pl.loop(0, n // step)
        def _(b):
            rows = pl.ds(pl.multiple_of(b * step, step), step)
            at = b * step + lax.broadcasted_iota(jnp.int32, (step, 1), 0)
            live = (at < length).astype(F32)
            own_ref[rows, :] = (
                live * (h1_ref[rows, :] + (feed_ref[rows, :] + rows_ref[7:8, :]))
            ).astype(BF16)

        for i in range(4):
            start(out_x[i])
        for i in range(4):
            start(out_core[i])
        keep.start()

    @pl.when((t == 4) | (t == 5))
    def _():
        for i in range(2):
            @pl.when(t == 4 + i)
            def _():
                recv(core2[i])

        value = weight_grad(gft_ref, h_ref[2 * (t - 4)])
        work2_ref[t - 4] = (value + land2_ref[t - 4].astype(F32)).astype(BF16)
        for i in range(2):
            @pl.when(t == 4 + i)
            def _():
                start(cross2[i])

    @pl.when(t >= 4)
    def _():
        @pl.loop(0, n // big)
        def _(b):
            rows = pl.ds(pl.multiple_of(b * big, big), big)
            dh = dot_nn(gf_ref[rows, :], w2_ref[0])
            df = (dh * slope_ref[k, rows, :].astype(F32)).astype(BF16)
            slope_ref[k, rows, :] = df
            sums_ref[pl.ds(8 + mine, 1), :] += jnp.sum(df.astype(F32), 0, keepdims=True)
            da2 = dot_nt(df, w1_ref[0])

            @pl.when(t == 4)
            def _():
                da2_ref[rows, :] = da2

            @pl.when(t > 4)
            def _():
                da2_ref[rows, :] += da2

    @pl.when((t == 4) | (t == 5))
    def _():
        for i in range(2):
            @pl.when(t == 4 + i)
            def _():
                core2[i].wait_send()

        stage1_ref[t - 4] = weight_grad(a2t_ref, slope_ref[k]).astype(BF16)
        for i in range(2):
            @pl.when(t == 4 + i)
            def _():
                start(core1[i])

    @pl.when(t >= 6)
    def _():
        for i in range(2):
            @pl.when(t == 6 + i)
            def _():
                recv(core1[i])
                recv(out_x[i])
                start(out_far[i])

        value = weight_grad(a2t_ref, slope_ref[k])
        d1_ref[t - 6] = (value + land1_ref[t - 6].astype(F32)).astype(BF16)

    @pl.when(t == 7)
    def _():
        @pl.loop(0, n // step)
        def _(b):
            rows = pl.ds(pl.multiple_of(b * step, step), step)
            at = b * step + lax.broadcasted_iota(jnp.int32, (step, 1), 0)
            live = (at < length).astype(F32)
            xhat, r = norm_parts(h1_ref[rows, :])
            da2 = da2_ref[rows, :]
            sums_ref[1:2, :] += jnp.sum(da2 * xhat, 0, keepdims=True)
            sums_ref[6:7, :] += jnp.sum(da2, 0, keepdims=True)
            dg = da2 * rows_ref[1:2, :]
            dv = r * (
                dg
                - jnp.mean(dg, -1, keepdims=True)
                - xhat * jnp.mean(dg * xhat, -1, keepdims=True)
            )
            dh1 = live * c_ref[rows, :].astype(F32) + dv
            dh1_ref[rows, :] = dh1
            gb = dh1.astype(BF16)
            gb_ref[rows, :] = gb
            gbt_ref[:, rows] = gb.T
            sums_ref[5:6, :] += jnp.sum(gb.astype(F32), 0, keepdims=True)

        recv(cross2[0], cross2[1])

        @pl.loop(0, Z_DEV)
        def _(z):
            for i in range(2):
                d2_ref[i, z] = (
                    work2_ref[i, z, y].astype(F32) + cross2_ref[i, z].astype(F32)
                ).astype(BF16)

        for i in range(2, 4):
            recv(out_x[i])
            start(out_far[i])
        for i in range(4):
            recv(out_core[i], out_far[i])
        links.sent(*core2)
        keep.wait()


def run_fused_feed_forward(lengths, cot, a2, a2t, h1, g1, g2, rows):
    n = cot.shape[1]
    groups, hidden = g1.shape[0], g1.shape[-1]
    depth = D // (Z_DEV * Y_DEV)
    halves = (2, Z_DEV, Y_DEV, depth, hidden)
    weight = pl.BlockSpec((1, D, hidden), lambda t: (group_order(t % 4), 0, 0))
    return pl.pallas_call(
        fused_feed_forward,
        grid=(2 * groups,),
        in_specs=[SMEM_WHOLE, ANY_WHOLE] + [VMEM_WHOLE] * 3 + [weight, weight, VMEM_WHOLE],
        out_specs=[ANY_WHOLE] + [VMEM_WHOLE] * 6,
        out_shape=[
            shaped(BF16, groups, n, D), shaped(BF16, *halves),
            shaped(BF16, 2, Z_DEV, depth, hidden), shaped(F32, n, D), shaped(BF16, n, D),
            shaped(BF16, D, n), shaped(F32, 16, D),
        ],
        scratch_shapes=[
            pltpu.VMEM((n, D), BF16), pltpu.VMEM((D, n), BF16), pltpu.VMEM((n, D), F32),
            pltpu.VMEM((groups, n, hidden), BF16),
            pltpu.VMEM((groups, n, hidden), BF16),
            pltpu.VMEM(halves, BF16), pltpu.VMEM(halves, BF16), pltpu.VMEM(halves, BF16),
            pltpu.VMEM(halves, BF16),
            pltpu.VMEM((2, Z_DEV, depth, hidden), BF16), pltpu.VMEM((n, D), BF16),
            pltpu.VMEM((n, D), BF16),
            pltpu.SemaphoreType.DMA((18,)), pltpu.SemaphoreType.DMA((18,)),
            pltpu.SemaphoreType.DMA((2,)),
        ],
        compiler_params=pltpu.CompilerParams(
            vmem_limit_bytes=VMEM_LIMIT, collective_id=1, has_side_effects=True
        ),
        name="fused_feed_forward",
    )(lengths, cot, a2, a2t, h1, g1, g2, rows)


class Reduce:
    def __init__(self, links, place, work, acc, cross_ref, far_ref, last_ref, side_ref):
        self.place, self.work, self.acc = place, work, acc
        self.cross_ref, self.far_ref = cross_ref, far_ref
        self.last_ref, self.side_ref = last_ref, side_ref
        zs = place.zs
        self.y = []
        if cross_ref is not None:
            self.y = [
                [
                    links.add(
                        place.to_y, work(s, zs[j], place.other_y), cross_ref.at[s, zs[j]]
                    )
                    for j in (1, 2, 3, 0)
                ]
                for s in range(2)
            ]
        self.z = [
            [
                links.add(place.to_z[j], acc(s, zs[j]), far_ref.at[s, j - 1])
                for j in range(1, 4)
            ]
            for s in range(2)
        ]
        self.x = links.add(place.to_x, last_ref, side_ref)

    def fold_y(self, s):
        for i, j in enumerate((1, 2, 3, 0)):
            z = self.place.zs[j]
            recv(self.y[s][i])
            value = self.work(s, z, self.place.y)[...].astype(F32)
            self.acc(s, z)[...] = (value + self.cross_ref[s, z].astype(F32)).astype(BF16)
            if j:
                start(self.z[s][j - 1])

    def own(self, s):
        recv(self.z[s])
        far = self.far_ref
        return self.acc(s, self.place.z)[...].astype(F32) + (
            far[s, 0].astype(F32) + far[s, 1].astype(F32) + far[s, 2].astype(F32)
        )

    def send_x(self):
        self.last_ref[...] = self.own(1).astype(BF16)
        start(self.x)

    def total(self):
        value = self.own(0)
        recv(self.x)
        return value + self.side_ref[...].astype(F32)


def fused_backward(
    tokens_ref, gq_ref, gw_ref, rows_ref, dh1_ref, gb_ref, gbt_ref, q_ref, v_ref, kt_ref,
    p_ref, o_ref, a1t_ref, d1_ref, d2_ref, early_ref,
    out_ref, part0_ref, partw_ref, part1_ref, part2_ref, total_ref,
    do_ref, delta_ref, dqt_ref, dqkv_ref, da1_ref, own_ref, bqv_ref,
    work1_ref, cross1_ref, far1_ref, last1_ref, side1_ref,
    far2_ref, last2_ref, side2_ref,
    stagew_ref, landw_ref, workw_ref, crossw_ref, farw_ref, lastw_ref, sidew_ref,
    stage0_ref, land0_ref, work0_ref, cross0_ref, far0_ref, last0_ref, side0_ref,
    sums_ref, sumland_ref,
    send_sem, recv_sem, local_sem,
):
    t = pl.program_id(0)
    n = own_ref.shape[0]
    width = gw_ref.shape[-1]
    depth = part0_ref.shape[0]
    heads = width // HEAD_DIM
    step = n // 4
    place = Place()
    y = place.y
    links = Links(send_sem, recv_sem)
    k, b = group_and_block(t)
    mine = place.group(k)
    out_x, out_core, out_far = [], [], []
    for i in range(4):
        rows = pl.ds(i * step, step)
        mine_there = out_ref.at[place.t, rows]
        far = out_ref.at[place.ts[2], rows]
        out_x.append(links.add(place.to_x, own_ref.at[rows], mine_there))
        out_core.append(links.add(place.to_core, own_ref.at[rows], mine_there))
        out_far.append(links.add(place.to_core, far, far))
    keeps = [
        pltpu.make_async_copy(
            own_ref.at[pl.ds(i * step, step)],
            out_ref.at[place.t, pl.ds(i * step, step)],
            local_sem.at[i],
        )
        for i in range(4)
    ]
    fetch = pltpu.make_async_copy(tokens_ref.at[place.t], own_ref, local_sem.at[4])
    corew = [links.add(place.to_core, stagew_ref.at[i], landw_ref.at[i]) for i in range(2)]
    core0 = [links.add(place.to_core, stage0_ref.at[i], land0_ref.at[i]) for i in range(2)]
    seg1 = Reduce(
        links, place, lambda s, z, y: d1_ref.at[s, z, y], lambda s, z: work1_ref.at[s, z],
        cross1_ref, far1_ref, last1_ref, side1_ref,
    )
    seg2 = Reduce(
        links, place, None, lambda s, z: d2_ref.at[s, z], None, far2_ref, last2_ref, side2_ref
    )
    segw = Reduce(
        links, place, lambda s, z, y: workw_ref.at[s, z, y],
        lambda s, z: workw_ref.at[s, z, y],
        crossw_ref, farw_ref, lastw_ref, sidew_ref,
    )
    seg0 = Reduce(
        links, place, lambda s, z, y: work0_ref.at[s, z, y],
        lambda s, z: work0_ref.at[s, z, y],
        cross0_ref, far0_ref, last0_ref, side0_ref,
    )
    sum_core, sum_x, sum_y, *sum_z = [
        links.add(to, sums_ref.at[min(i, 3)], sumland_ref.at[i])
        for i, to in enumerate([place.to_core, place.to_x, place.to_y] + place.to_z[1:])
    ]

    def when(now):
        return pl.when(t == now)

    @when(0)
    def _():
        fetch.start()
        place.greet()
        start(seg1.y[1], seg1.y[0], seg2.z[1], seg2.z[0])
        bqv_ref[...] = jnp.zeros_like(bqv_ref)
        sums_ref[0] = early_ref[...]
        da1_ref[...] = jnp.zeros_like(da1_ref)
        fetch.wait()

    @when(3)
    def _():
        seg1.fold_y(1)

    @when(7)
    def _():
        seg1.fold_y(0)
        seg2.send_x()

    @when(9)
    def _():
        recv(out_x[0])
        start(out_far[0])

    @when(10)
    def _():
        segw.fold_y(1)
        segw.fold_y(0)

    @when(12)
    def _():
        seg1.send_x()

    @pl.when(t < 4)
    def _():
        pick = (
            lax.broadcasted_iota(jnp.int32, (16, width), 1) // HEAD_DIM
            == lax.broadcasted_iota(jnp.int32, (16, width), 0)
        ).astype(BF16)

        @pl.loop(0, n // step)
        def _(i):
            rows = pl.ds(pl.multiple_of(i * step, step), step)
            do = dot_nn(gb_ref[rows, :], gw_ref[0]).astype(BF16)
            do_ref[k, rows, :] = do
            prod = do.astype(F32) * o_ref[0, rows, :].astype(F32)
            high = prod.astype(BF16)
            low = (prod - high.astype(F32)).astype(BF16)
            delta_ref[k, :, rows] = dot_nt(pick, high) + dot_nt(pick, low)

        dqt_ref[k] = jnp.zeros(dqt_ref.shape[1:], F32)
        value = dot_nn(gbt_ref[...], o_ref[0]).reshape(Z_DEV, Y_DEV, depth, width)
        for i in range(2):
            @when(i)
            def _():
                stagew_ref[i] = value.astype(BF16)
                start(corew[i])

            @when(2 + i)
            def _():
                recv(corew[i])
                workw_ref[i] = (value + landw_ref[i].astype(F32)).astype(BF16)
                start(segw.y[i])

    for bb in range(4):
        @pl.when(b == bb)
        def _():
            first, last = bb * step, (bb + 1) * step
            do = do_ref[k, first:, :]
            q = q_ref[0, first:, :]
            v = v_ref[0, first:last, :]
            dk, dv = None, None
            for h in range(heads):
                lanes = head_mask((1, width), h)
                zero = jnp.zeros((), BF16)
                p = p_ref[0, h, :, first:]
                dp = dot_nt(jnp.where(lanes, v, zero), do)
                ds = (p.astype(F32) * (dp - delta_ref[k, h : h + 1, first:])).astype(BF16)
                part = dot_nn(p, jnp.where(lanes, do, zero))
                dv = part if dv is None else dv + part
                part = dot_nn(ds, jnp.where(lanes, q, zero))
                dk = part if dk is None else dk + part
                head = slice(h * HEAD_DIM, (h + 1) * HEAD_DIM)
                dqt_ref[k, head, first:] += dot_nn(kt_ref[0, head, first:last], ds)
            dk = dk.astype(BF16)
            dv = dv.astype(BF16)
            dq = (dqt_ref[k, :, first:last] * HEAD_DIM ** -0.5).astype(BF16).T
            dqkv_ref[k, first:last, :width] = dq
            dqkv_ref[k, first:last, width : 2 * width] = dk
            dqkv_ref[k, first:last, 2 * width :] = dv
            bqv_ref[mine, 0:1, :] += jnp.sum(dq.astype(F32), 0, keepdims=True)
            bqv_ref[mine, 1:2, :] += jnp.sum(dv.astype(F32), 0, keepdims=True)
            da1_ref[first:last, :] += dot_nt(dqkv_ref[k, first:last, :], gq_ref[0])

    @pl.when((t == 3) | (t > 12))
    def _():
        rows = pl.ds(pl.multiple_of(b * step, step), step)
        xhat, r = norm_parts(own_ref[rows, :].astype(F32))
        da1 = da1_ref[rows, :]
        sums_ref[0, 0:1, :] += jnp.sum(da1 * xhat, 0, keepdims=True)
        sums_ref[0, 2:3, :] += jnp.sum(da1, 0, keepdims=True)
        dg = da1 * rows_ref[0:1, :]
        dv = r * (
            dg
            - jnp.mean(dg, -1, keepdims=True)
            - xhat * jnp.mean(dg * xhat, -1, keepdims=True)
        )
        own_ref[rows, :] = (dh1_ref[rows, :] + dv).astype(BF16)
        for i in range(4):
            @pl.when(b == i)
            def _():
                start(out_x[i], out_core[i])
                keeps[i].start()

    @pl.when((t == 6) | (t == 9) | (t == 12) | (t == 15))
    def _():
        value = dot_nn(a1t_ref[...], dqkv_ref[k]).reshape(Z_DEV, Y_DEV, depth, 3 * width)
        for i in range(2):
            @when(6 + 3 * i)
            def _():
                stage0_ref[i] = value.astype(BF16)
                start(core0[i])

            @when(12 + 3 * i)
            def _():
                recv(core0[i])
                work0_ref[i] = (value + land0_ref[i].astype(F32)).astype(BF16)
                start(seg0.y[i])

    @when(15)
    def _():
        for s in range(4):
            sums_ref[0, 3:5, s * width : (s + 1) * width] = bqv_ref[s, 0:2, :]
        start(sum_core)
        seg0.fold_y(0)
        segw.send_x()
        recv(sum_core)
        sums_ref[1] = sums_ref[0] + sumland_ref[0]
        start(sum_x)
        recv(out_x[1])
        start(out_far[1])
        part2_ref[...] = seg2.total()
        recv(sum_x)
        sums_ref[2] = sums_ref[1] + sumland_ref[1]
        start(sum_y)
        recv(out_x[2])
        start(out_far[2])
        seg0.fold_y(1)
        recv(sum_y)
        sums_ref[3] = sums_ref[2] + sumland_ref[2]
        start(sum_z)
        part1_ref[...] = seg1.total()
        partw_ref[...] = segw.total()
        seg0.send_x()
        recv(out_x[3])
        start(out_far[3])
        recv(sum_z)
        total_ref[...] = (sums_ref[3] + sumland_ref[3]) + (sumland_ref[4] + sumland_ref[5])
        part0_ref[...] = seg0.total()
        for i in range(4):
            recv(out_core[i], out_far[i])
            keeps[i].wait()
        links.sent()


def group_and_block(t):
    later = t - 4
    k = jnp.where(t < 4, group_order(t % 4), group_order(jnp.maximum(later, 0) // 3))
    b = jnp.where(t < 4, 0, 1 + jnp.maximum(later, 0) % 3)
    return k, b


def run_fused_backward(
    tokens, gq, gw, rows, dh1, gb, gbt, q, v, kt, p, o, a1t, d1, d2, early
):
    groups, n, _ = tokens.shape
    width = gw.shape[-1]
    heads = width // HEAD_DIM
    hidden = d1.shape[-1]
    depth = D // (Z_DEV * Y_DEV)
    step = n // 4

    def by_group(*shape):
        return pl.BlockSpec(
            (1,) + shape, lambda t: (group_and_block(t)[0],) + (0,) * len(shape)
        )

    p_spec = pl.BlockSpec(
        (1, heads, step, n),
        lambda t: (group_and_block(t)[0], 0, group_and_block(t)[1], 0),
    )

    def early_group(*shape):
        return pl.BlockSpec(
            (1,) + shape, lambda t: (group_order(jnp.minimum(t, 3)),) + (0,) * len(shape)
        )

    copies = 12 + 4 + 3 * 15 + 7 + 6

    def landing(lanes):
        return [
            pltpu.VMEM((2, Z_DEV, depth, lanes), BF16),
            pltpu.VMEM((2, 3, depth, lanes), BF16),
            pltpu.VMEM((depth, lanes), BF16), pltpu.VMEM((depth, lanes), BF16),
        ]

    def working(lanes):
        return [pltpu.VMEM((2, Z_DEV, Y_DEV, depth, lanes), BF16)] * 3

    return pl.pallas_call(
        fused_backward,
        grid=(4 * groups,),
        in_specs=[
            ANY_WHOLE, by_group(D, 3 * width), early_group(D, width), VMEM_WHOLE, VMEM_WHOLE,
            VMEM_WHOLE, VMEM_WHOLE, by_group(n, width), by_group(n, width),
            by_group(width, n), p_spec, early_group(n, width),
            VMEM_WHOLE, VMEM_WHOLE, VMEM_WHOLE, VMEM_WHOLE,
        ],
        out_specs=[ANY_WHOLE] + [VMEM_WHOLE] * 5,
        out_shape=[
            shaped(BF16, groups, n, D), shaped(F32, depth, 3 * width),
            shaped(F32, depth, width), shaped(F32, depth, hidden),
            shaped(F32, depth, hidden), shaped(F32, 16, D),
        ],
        scratch_shapes=[
            pltpu.VMEM((groups, n, width), BF16),
            pltpu.VMEM((groups, 16, n), F32), pltpu.VMEM((groups, width, n), F32),
            pltpu.VMEM((groups, n, 3 * width), BF16), pltpu.VMEM((n, D), F32),
            pltpu.VMEM((n, D), BF16), pltpu.VMEM((groups, 8, width), F32),
        ]
        + landing(hidden)[:1] + landing(hidden) + landing(hidden)[1:]
        + working(width) + landing(width)
        + working(3 * width) + landing(3 * width)
        + [
            pltpu.VMEM((4, 16, D), F32), pltpu.VMEM((6, 16, D), F32),
            pltpu.SemaphoreType.DMA((copies,)), pltpu.SemaphoreType.DMA((copies,)),
            pltpu.SemaphoreType.DMA((5,)),
        ],
        compiler_params=pltpu.CompilerParams(
            vmem_limit_bytes=VMEM_LIMIT, collective_id=2, has_side_effects=True
        ),
        name="fused_backward",
    )(tokens, gq, gw, rows, dh1, gb, gbt, q, v, kt, p, o, a1t, d1, d2, early)


def place_gradients(
    tie_ref, sums_ref, part0_ref, partw_ref, part1_ref, part2_ref, near_out, near_grad,
    far_out, far_grad, gains_ref, bias_ref, in_ref, out_ref, expand_ref, project_ref,
    sem,
):
    copies = [
        pltpu.make_async_copy(near_out, far_out, sem.at[0]),
        pltpu.make_async_copy(near_grad, far_grad, sem.at[1]),
    ]
    for copy in copies:
        copy.start()
    own = gains_ref.shape[-1]
    width = partw_ref.shape[-1]
    first = (lax.axis_index("dp") * 4 + lax.axis_index("tensor")) * own
    feature = lax.broadcasted_iota(jnp.int32, (D, 128), 0)
    lane = lax.broadcasted_iota(jnp.int32, (D, 128), 1)
    chosen = ((feature == first + lane) & (lane < own)).astype(F32)
    sums = lax.dot_general(
        sums_ref[...], chosen, (((1,), (0,)), ((), ())),
        precision=lax.Precision.HIGHEST, preferred_element_type=F32,
    )[:, :own]
    s0, s1, s2, s3 = tie_ref[0], tie_ref[1], tie_ref[2], tie_ref[3]
    w_out = partw_ref[...].T
    w_project = part2_ref[...].T

    def at(source, wanted, value):
        return jnp.where(source == wanted, value, jnp.zeros_like(value))

    for s in range(NSRC):
        gains_ref[s, 0:1] = at(s, s0, sums[0:1])
        gains_ref[s, 1:2] = at(s, s2, sums[1:2])
        bias_ref[s, 0:3] = at(s, s0, sums[2:5])
        bias_ref[s, 3:4] = at(s, s1, sums[5:6])
        bias_ref[s, 4:5] = at(s, s2, sums[6:7])
        bias_ref[s, 5:6] = at(s, s3, sums[7:8])
        bias_ref[s, 6:10] = at(s, s2, sums[8:12])
        for j in range(3):
            in_ref[s, j] = at(s, s0, part0_ref[:, j * width : (j + 1) * width])
        out_ref[s] = at(s, s1, w_out)
        expand_ref[s] = at(s, s2, part1_ref[...])
        project_ref[s] = at(s, s3, w_project)
    for copy in copies:
        copy.wait()


def run_place_gradients(tie, sums, part0, partw, part1, part2, out, grad, like):
    return pl.pallas_call(
        place_gradients,
        in_specs=[SMEM_WHOLE] + [VMEM_WHOLE] * 5 + [ANY_WHOLE] * 2,
        out_specs=[ANY_WHOLE] * 2 + [VMEM_WHOLE] * 6,
        out_shape=[shaped(BF16, *out.shape), shaped(BF16, *grad.shape)]
        + [shaped(F32, *item.shape) for item in like],
        scratch_shapes=[pltpu.SemaphoreType.DMA((2,))],
        compiler_params=pltpu.CompilerParams(vmem_limit_bytes=VMEM_LIMIT),
        name="place_gradients",
    )(tie, sums, part0, partw, part1, part2, out, grad)


def plain_step(
    tokens, lengths, tie_map, norm_gains, bias_rows, attention_in, attention_out,
    expand_weight, project_weight, cotangent,
):
    slot_rows = tokens.shape[0] // lengths.shape[0]
    me = lax.axis_index("tensor")
    in_local = lax.dynamic_index_in_dim(attention_in, tie_map[0], 0, keepdims=False)
    out_local = lax.dynamic_index_in_dim(attention_out, tie_map[1], 0, keepdims=False)
    expand_local = lax.dynamic_index_in_dim(expand_weight, tie_map[2], 0, keepdims=False)
    project_local = lax.dynamic_index_in_dim(project_weight, tie_map[3], 0, keepdims=False)
    local0 = jnp.concatenate([in_local, out_local.T[None]], 0)
    row_kinds = jnp.array([0, 0, 0, 1, 2, 3] + [2] * (FF // D), dtype=jnp.int32)
    gain_kinds = jnp.array([0, 2], dtype=jnp.int32)
    gain_pick = norm_gains[tie_map[gain_kinds], jnp.arange(2)]
    bias_pick = bias_rows[tie_map[row_kinds], jnp.arange(row_kinds.shape[0])]
    vectors = jnp.concatenate([gain_pick, bias_pick], 0)
    x = lax.dynamic_slice_in_dim(tokens, me * slot_rows, slot_rows, 0)
    cot = lax.dynamic_slice_in_dim(cotangent, me * slot_rows, slot_rows, 0)
    length = lax.dynamic_slice_in_dim(lengths, me, 1, 0)
    rows = lax.all_gather(vectors, ("dp", "tensor"), axis=1, tiled=True).astype(F32)
    rows = jnp.concatenate([rows, jnp.zeros((4, D), F32)], 0)

    def gathered(piece, axis):
        piece = lax.all_gather(piece, "dp", axis=axis, tiled=True)
        return lax.all_gather(piece, "tensor", axis=0)

    g0 = gathered(local0, 1)
    g1 = gathered(expand_local, 0)
    g2 = gathered(project_local.T, 0)
    groups, width = g0.shape[0], g0.shape[-1]
    bqv = rows[3:5].reshape(2, groups, width).transpose(1, 0, 2)
    q, v, kt, p, o, a1t, h1, a2, a2t = run_attention_forward(length, x, g0, rows, bqv)
    out, d1, d2, dh1, gb, gbt, sums = run_feed_forward(length, cot, a2, a2t, h1, g1, g2, rows)
    d0, xg, sums_in, sums_qv = run_attention_backward(
        x, g0, rows, dh1, gb, gbt, q, v, kt, p, o, a1t
    )
    layer_out = lax.all_gather(out, "tensor", axis=0, tiled=True)
    tokens_grad = lax.all_gather(xg, "tensor", axis=0, tiled=True)

    def scattered(piece, axis):
        piece = lax.psum_scatter(piece, "tensor", scatter_dimension=0)
        return lax.psum_scatter(piece, "dp", scatter_dimension=axis, tiled=True).astype(F32)

    part0 = scattered(d0, 1)
    part1 = scattered(d1, 0)
    part2 = scattered(d2, 0)
    qv = sums_qv[:, :2].transpose(1, 0, 2).reshape(2, D)
    sums = jnp.concatenate(
        [sums_in[0:1], sums[1:2], sums_in[1:2], qv, sums[5:12]], 0
    )
    sums = lax.psum_scatter(sums, ("dp", "tensor"), scatter_dimension=1, tiled=True)
    return layer_out, tokens_grad, *placed(tie_map, sums, part0, part1, part2)


def fused_step(
    tokens, lengths, tie_map, norm_gains, bias_rows, attention_in, attention_out,
    expand_weight, project_weight, cotangent,
):
    slots = lengths.shape[0]
    tokens = tokens.reshape(slots, -1, D)
    cotangent = cotangent.reshape(slots, -1, D)
    gq, gw, g1, g2, rows, q, v, kt, p, o, a1t, h1, a2, a2t = run_fused_forward(
        tie_map, lengths, tokens, norm_gains, bias_rows, attention_in, attention_out,
        expand_weight, project_weight,
    )
    g1 = g1.reshape(g1.shape[0], D, -1)
    g2 = g2.reshape(g2.shape[0], D, -1)
    out, d1, d2, dh1, gb, gbt, early = run_fused_feed_forward(
        lengths, cotangent, a2, a2t, h1, g1, g2, rows
    )
    grad, part0, partw, part1, part2, sums = run_fused_backward(
        tokens, gq, gw, rows, dh1, gb, gbt, q, v, kt, p, o, a1t, d1, d2, early
    )
    out, grad, *placed_grads = run_place_gradients(
        tie_map, sums, part0, partw, part1, part2, out, grad,
        (norm_gains, bias_rows, attention_in, attention_out, expand_weight, project_weight),
    )
    return out.reshape(-1, D), grad.reshape(-1, D), *placed_grads


def placed(tie_map, sums, part0, part1, part2):
    source = jnp.arange(NSRC, dtype=jnp.int32)

    def place(piece, which):
        pick = (source == tie_map[which]).reshape((NSRC,) + (1,) * piece.ndim)
        return jnp.where(pick, piece[None], 0.0)

    def place_rows(piece, kinds):
        pick = source[:, None] == tie_map[jnp.array(kinds, dtype=jnp.int32)][None, :]
        return jnp.where(pick[:, :, None], piece[None], 0.0)

    return (
        place_rows(sums[:2], [0, 2]),
        place_rows(sums[2:], [0, 0, 0, 1, 2, 3] + [2] * (FF // D)),
        place(part0[:3], 0),
        place(part0[3].T, 1),
        place(part1, 2),
        place(part2.T, 3),
    )


def solution(mesh):
    fused = mesh.shape["dp"] == Z_DEV * Y_DEV and mesh.shape["tensor"] == X_DEV * C_DEV
    return jax.shard_map(
        fused_step if fused else plain_step,
        mesh=mesh,
        in_specs=(
            P("dp", None),
            P("dp"),
            P(),
            P(None, None, ("dp", "tensor")),
            P(None, None, ("dp", "tensor")),
            P(None, None, "dp", "tensor"),
            P(None, "tensor", "dp"),
            P(None, "dp", "tensor"),
            P(None, "tensor", "dp"),
            P("dp", None),
        ),
        out_specs=(
            P("dp", None),
            P("dp", None),
            P(None, None, ("dp", "tensor")),
            P(None, None, ("dp", "tensor")),
            P(None, None, "dp", "tensor"),
            P(None, "tensor", "dp"),
            P(None, "dp", "tensor"),
            P(None, "tensor", "dp"),
        ),
        check_vma=False,
    )
```

```python
import jax
import jax.numpy as jnp
from jax import lax
from jax.experimental import pallas as pl
from jax.experimental.pallas import tpu as pltpu
from jax.sharding import PartitionSpec as P

D = 768
HEAD_DIM = 64
FF = 3072
NSRC = 4
EPS = 1e-05
MASKED = -1e30
F32 = jnp.float32
BF16 = jnp.bfloat16
VMEM_LIMIT = 60 * 1024 * 1024


def dot_nn(a, b):
    return lax.dot_general(a, b, (((1,), (0,)), ((), ())), preferred_element_type=F32)


def dot_nt(a, b):
    return lax.dot_general(a, b, (((1,), (1,)), ((), ())), preferred_element_type=F32)


def norm_parts(v):
    center = jnp.mean(v, -1, keepdims=True)
    centered = v - center
    r = lax.rsqrt(jnp.mean(centered * centered, -1, keepdims=True) + EPS)
    return centered * r, r


def head_mask(shape, h):
    lane = lax.broadcasted_iota(jnp.int32, shape, 1)
    return (lane >= h * HEAD_DIM) & (lane < (h + 1) * HEAD_DIM)


def blocks(total, size):
    return [slice(i * size, (i + 1) * size) for i in range(total // size)]


def attention_forward(
    len_ref, x_ref, g_ref, rows_ref, bqv_ref,
    q_ref, v_ref, kt_ref, p_ref, o_ref, a1t_ref, h1_ref, a2_ref, a2t_ref,
    a1_ref, k_ref, vt_ref, ot_ref, attn_ref,
):
    t = pl.program_id(0)
    n = x_ref.shape[0]
    width = g_ref.shape[-1]
    heads = width // HEAD_DIM
    step = 256
    length = len_ref[0]

    @pl.when(t == 0)
    def _():
        @pl.loop(0, n // step)
        def _(b):
            rows = pl.ds(pl.multiple_of(b * step, step), step)
            xhat, _ = norm_parts(x_ref[rows, :].astype(F32))
            a1 = xhat * rows_ref[0:1, :] + rows_ref[2:3, :]
            a1_ref[rows, :] = a1.astype(BF16)
            a1t_ref[:, rows] = a1.astype(BF16).T
            attn_ref[rows, :] = x_ref[rows, :].astype(F32) + rows_ref[5:6, :]

    @pl.loop(0, n // step)
    def _(b):
        rows = pl.ds(pl.multiple_of(b * step, step), step)
        a1 = a1_ref[rows, :]
        q = (dot_nn(a1, g_ref[0, 0]) + bqv_ref[0, 0:1, :]).astype(BF16)
        q_ref[0, rows, :] = q * jnp.asarray(HEAD_DIM ** -0.5, BF16)
        k = dot_nn(a1, g_ref[0, 1]).astype(BF16)
        k_ref[rows, :] = k
        kt_ref[0, :, rows] = k.T
        v = (dot_nn(a1, g_ref[0, 2]) + bqv_ref[0, 1:2, :]).astype(BF16)
        v_ref[0, rows, :] = v
        vt_ref[:, rows] = v.T

    for h in range(heads):
        k = k_ref[...]
        k = jnp.where(head_mask(k.shape, h), k, jnp.zeros_like(k))
        for b in range(n // step):
            first, last = b * step, (b + 1) * step
            q = q_ref[0, first:last, :]
            key = lax.broadcasted_iota(jnp.int32, (last, step), 0)
            query = lax.broadcasted_iota(jnp.int32, (step, step), 1) + first
            s = dot_nt(k[:last], q)
            near = jnp.where(
                (key[first:] <= query) & (key[first:] < length), s[first:], MASKED
            )
            if b:
                far = jnp.where(key[:first] < length, s[:first], MASKED)
                top = jnp.maximum(
                    jnp.max(far, 0, keepdims=True), jnp.max(near, 0, keepdims=True)
                )
                e_far = jnp.exp(far - top)
                e_near = jnp.exp(near - top)
                total = jnp.sum(e_far, 0, keepdims=True) + jnp.sum(e_near, 0, keepdims=True)
                scale = 1.0 / total
                p_ref[0, h, :first, first:last] = (e_far * scale).astype(BF16)
            else:
                top = jnp.max(near, 0, keepdims=True)
                e_near = jnp.exp(near - top)
                scale = 1.0 / jnp.sum(e_near, 0, keepdims=True)
            p_ref[0, h, first:last, first:last] = (e_near * scale).astype(BF16)
            ot_ref[h * HEAD_DIM : (h + 1) * HEAD_DIM, first:last] = dot_nn(
                vt_ref[h * HEAD_DIM : (h + 1) * HEAD_DIM, :last],
                p_ref[0, h, :last, first:last],
            ).astype(BF16)

    @pl.loop(0, n // step)
    def _(b):
        rows = pl.ds(pl.multiple_of(b * step, step), step)
        o = ot_ref[:, rows].T
        o_ref[0, rows, :] = o
        attn_ref[rows, :] += dot_nt(o, g_ref[0, 3])

    @pl.when(t == pl.num_programs(0) - 1)
    def _():
        @pl.loop(0, n // step)
        def _(b):
            rows = pl.ds(pl.multiple_of(b * step, step), step)
            h1 = attn_ref[rows, :]
            h1_ref[rows, :] = h1
            xhat, _ = norm_parts(h1)
            a2 = (xhat * rows_ref[1:2, :] + rows_ref[6:7, :]).astype(BF16)
            a2_ref[rows, :] = a2
            a2t_ref[:, rows] = a2.T


SQRT_2_PI = 0.7978845608028654


def feed_forward_both(
    len_ref, c_ref, a2_ref, a2t_ref, h1_ref, w1_ref, w2_ref, rows_ref,
    out_ref, d1_ref, d2_ref, dh1_ref, gb_ref, gbt_ref, sums_ref,
    gf_ref, gft_ref, feed_ref, da2_ref, h_ref, df_ref,
):
    t = pl.program_id(0)
    n = c_ref.shape[0]
    step = 256
    length = len_ref[0]

    @pl.when(t == 0)
    def _():
        sums_ref[...] = jnp.zeros_like(sums_ref)

        @pl.loop(0, n // step)
        def _(b):
            rows = pl.ds(pl.multiple_of(b * step, step), step)
            place = b * step + lax.broadcasted_iota(jnp.int32, (step, 1), 0)
            live = (place < length).astype(F32)
            g = (c_ref[rows, :].astype(F32) * live).astype(BF16)
            gf_ref[rows, :] = g
            gft_ref[:, rows] = g.T
            sums_ref[7:8, :] += jnp.sum(g.astype(F32), 0, keepdims=True)

    bias = rows_ref[pl.ds(8 + t, 1), :]

    @pl.loop(0, n // step)
    def _(b):
        rows = pl.ds(pl.multiple_of(b * step, step), step)
        f = dot_nn(a2_ref[rows, :], w1_ref[0]) + bias
        dh = dot_nn(gf_ref[rows, :], w2_ref[0])
        f2 = f * f
        th = jnp.tanh(f * (SQRT_2_PI + (SQRT_2_PI * 0.044715) * f2))
        half = 0.5 + 0.5 * th
        h = (f * half).astype(BF16)
        slope = half + f * (0.5 - 0.5 * th * th) * (
            SQRT_2_PI + (3 * SQRT_2_PI * 0.044715) * f2
        )
        df = (dh * slope).astype(BF16)
        h_ref[rows, :] = h
        df_ref[rows, :] = df
        sums_ref[pl.ds(8 + t, 1), :] += jnp.sum(df.astype(F32), 0, keepdims=True)
        feed = dot_nt(h, w2_ref[0])
        da2 = dot_nt(df, w1_ref[0])

        @pl.when(t == 0)
        def _():
            feed_ref[rows, :] = feed
            da2_ref[rows, :] = da2

        @pl.when(t > 0)
        def _():
            feed_ref[rows, :] += feed
            da2_ref[rows, :] += da2

    @pl.loop(0, D // step)
    def _(b):
        rows = pl.ds(pl.multiple_of(b * step, step), step)
        d1_ref[0, rows, :] = dot_nn(a2t_ref[rows, :], df_ref[...]).astype(BF16)
        d2_ref[0, rows, :] = dot_nn(gft_ref[rows, :], h_ref[...]).astype(BF16)

    @pl.when(t == pl.num_programs(0) - 1)
    def _():
        @pl.loop(0, n // step)
        def _(b):
            rows = pl.ds(pl.multiple_of(b * step, step), step)
            place = b * step + lax.broadcasted_iota(jnp.int32, (step, 1), 0)
            live = (place < length).astype(F32)
            h1 = h1_ref[rows, :]
            out_ref[rows, :] = (live * (h1 + (feed_ref[rows, :] + rows_ref[7:8, :]))).astype(BF16)
            xhat, r = norm_parts(h1)
            da2 = da2_ref[rows, :]
            sums_ref[1:2, :] += jnp.sum(da2 * xhat, 0, keepdims=True)
            sums_ref[6:7, :] += jnp.sum(da2, 0, keepdims=True)
            dg = da2 * rows_ref[1:2, :]
            dv = r * (
                dg
                - jnp.mean(dg, -1, keepdims=True)
                - xhat * jnp.mean(dg * xhat, -1, keepdims=True)
            )
            dh1 = live * c_ref[rows, :].astype(F32) + dv
            dh1_ref[rows, :] = dh1
            gb = dh1.astype(BF16)
            gb_ref[rows, :] = gb
            gbt_ref[:, rows] = gb.T
            sums_ref[5:6, :] += jnp.sum(gb.astype(F32), 0, keepdims=True)


def attention_backward(
    x_ref, g_ref, rows_ref, dh1_ref, gb_ref, gbt_ref, q_ref, v_ref, kt_ref, p_ref,
    o_ref, a1t_ref,
    d0_ref, xg_ref, sums_ref, bqv_ref,
    do_ref, delta_ref, dqt_ref, dq_ref, dk_ref, dv_ref, da1_ref,
):
    t = pl.program_id(0)
    n = x_ref.shape[0]
    width = g_ref.shape[-1]
    heads = width // HEAD_DIM
    step = 256
    pick = (
        lax.broadcasted_iota(jnp.int32, (16, width), 1) // HEAD_DIM
        == lax.broadcasted_iota(jnp.int32, (16, width), 0)
    ).astype(BF16)

    @pl.loop(0, n // step)
    def _(b):
        rows = pl.ds(pl.multiple_of(b * step, step), step)
        do = dot_nn(gb_ref[rows, :], g_ref[0, 3]).astype(BF16)
        do_ref[rows, :] = do
        prod = do.astype(F32) * o_ref[0, rows, :].astype(F32)
        high = prod.astype(BF16)
        low = (prod - high.astype(F32)).astype(BF16)
        delta_ref[:, rows] = dot_nt(pick, high) + dot_nt(pick, low)

    dqt_ref[...] = jnp.zeros_like(dqt_ref)
    for b in range(n // step):
        first, last = b * step, (b + 1) * step
        do = do_ref[first:, :]
        q = q_ref[0, first:, :]
        v = v_ref[0, first:last, :]
        dk, dv = None, None
        for h in range(heads):
            mine = head_mask((1, width), h)
            zero = jnp.zeros((), BF16)
            p = p_ref[0, h, first:last, first:]
            dp = dot_nt(jnp.where(mine, v, zero), do)
            ds = (p.astype(F32) * (dp - delta_ref[h : h + 1, first:])).astype(BF16)
            part = dot_nn(p, jnp.where(mine, do, zero))
            dv = part if dv is None else dv + part
            part = dot_nn(ds, jnp.where(mine, q, zero))
            dk = part if dk is None else dk + part
            head = slice(h * HEAD_DIM, (h + 1) * HEAD_DIM)
            dqt_ref[head, first:] += dot_nn(kt_ref[0, head, first:last], ds)
        dk_ref[first:last, :] = dk.astype(BF16)
        dv_ref[first:last, :] = dv.astype(BF16)

    @pl.when(t == 0)
    def _():
        da1_ref[...] = jnp.zeros_like(da1_ref)

    bqv_ref[...] = jnp.zeros_like(bqv_ref)

    @pl.loop(0, n // step)
    def _(b):
        rows = pl.ds(pl.multiple_of(b * step, step), step)
        dq = (dqt_ref[:, rows] * HEAD_DIM ** -0.5).astype(BF16).T
        dk = dk_ref[rows, :]
        dv = dv_ref[rows, :]
        dq_ref[rows, :] = dq
        bqv_ref[0, 0:1, :] += jnp.sum(dq.astype(F32), 0, keepdims=True)
        bqv_ref[0, 1:2, :] += jnp.sum(dv.astype(F32), 0, keepdims=True)
        da1_ref[rows, :] += (
            dot_nt(dq, g_ref[0, 0]) + dot_nt(dk, g_ref[0, 1]) + dot_nt(dv, g_ref[0, 2])
        )

    @pl.loop(0, D // step)
    def _(b):
        rows = pl.ds(pl.multiple_of(b * step, step), step)
        a1t = a1t_ref[rows, :]
        d0_ref[0, 0, rows, :] = dot_nn(a1t, dq_ref[...]).astype(BF16)
        d0_ref[0, 1, rows, :] = dot_nn(a1t, dk_ref[...]).astype(BF16)
        d0_ref[0, 2, rows, :] = dot_nn(a1t, dv_ref[...]).astype(BF16)
        d0_ref[0, 3, rows, :] = dot_nn(gbt_ref[rows, :], o_ref[0]).astype(BF16)

    @pl.when(t == pl.num_programs(0) - 1)
    def _():
        sums_ref[...] = jnp.zeros_like(sums_ref)

        @pl.loop(0, n // step)
        def _(b):
            rows = pl.ds(pl.multiple_of(b * step, step), step)
            xhat, r = norm_parts(x_ref[rows, :].astype(F32))
            da1 = da1_ref[rows, :]
            sums_ref[0:1, :] += jnp.sum(da1 * xhat, 0, keepdims=True)
            sums_ref[1:2, :] += jnp.sum(da1, 0, keepdims=True)
            dg = da1 * rows_ref[0:1, :]
            dv = r * (
                dg
                - jnp.mean(dg, -1, keepdims=True)
                - xhat * jnp.mean(dg * xhat, -1, keepdims=True)
            )
            xg_ref[rows, :] = (dh1_ref[rows, :] + dv).astype(BF16)


def whole(*shape):
    return pl.BlockSpec(shape, lambda t: (0,) * len(shape))


def group(*shape):
    return pl.BlockSpec((1,) + shape, lambda t: (t,) + (0,) * len(shape))


def shaped(dtype, *shape):
    return jax.ShapeDtypeStruct(shape, dtype)


SMEM_WHOLE = pl.BlockSpec(memory_space=pltpu.SMEM)


def run_attention_forward(length, x, g0, rows, bqv):
    n = x.shape[0]
    groups, _, _, width = g0.shape
    heads = width // HEAD_DIM
    return pl.pallas_call(
        attention_forward,
        grid=(groups,),
        in_specs=[SMEM_WHOLE, whole(n, D), group(4, D, width), whole(16, D), group(2, width)],
        out_specs=[
            group(n, width), group(n, width), group(width, n), group(heads, n, n),
            group(n, width), whole(D, n), whole(n, D), whole(n, D), whole(D, n),
        ],
        out_shape=[
            shaped(BF16, groups, n, width), shaped(BF16, groups, n, width),
            shaped(BF16, groups, width, n), shaped(BF16, groups, heads, n, n),
            shaped(BF16, groups, n, width), shaped(BF16, D, n), shaped(F32, n, D),
            shaped(BF16, n, D), shaped(BF16, D, n),
        ],
        scratch_shapes=[
            pltpu.VMEM((n, D), BF16), pltpu.VMEM((n, width), BF16),
            pltpu.VMEM((width, n), BF16), pltpu.VMEM((width, n), BF16),
            pltpu.VMEM((n, D), F32),
        ],
        compiler_params=pltpu.CompilerParams(vmem_limit_bytes=VMEM_LIMIT),
        name="attention_forward",
    )(length, x, g0, rows, bqv)


def run_feed_forward(length, cot, a2, a2t, h1, g1, g2, rows):
    n = cot.shape[0]
    groups, _, width = g1.shape
    return pl.pallas_call(
        feed_forward_both,
        grid=(groups,),
        in_specs=[
            SMEM_WHOLE, whole(n, D), whole(n, D), whole(D, n), whole(n, D),
            group(D, width), group(D, width), whole(16, D),
        ],
        out_specs=[
            whole(n, D), group(D, width), group(D, width), whole(n, D), whole(n, D),
            whole(D, n), whole(16, D),
        ],
        out_shape=[
            shaped(BF16, n, D), shaped(BF16, groups, D, width), shaped(BF16, groups, D, width),
            shaped(F32, n, D), shaped(BF16, n, D), shaped(BF16, D, n), shaped(F32, 16, D),
        ],
        scratch_shapes=[
            pltpu.VMEM((n, D), BF16), pltpu.VMEM((D, n), BF16), pltpu.VMEM((n, D), F32),
            pltpu.VMEM((n, D), F32), pltpu.VMEM((n, width), BF16), pltpu.VMEM((n, width), BF16),
        ],
        compiler_params=pltpu.CompilerParams(vmem_limit_bytes=VMEM_LIMIT),
        name="feed_forward_both",
    )(length, cot, a2, a2t, h1, g1, g2, rows)


def run_attention_backward(x, g0, rows, dh1, gb, gbt, q, v, kt, p, o, a1t):
    n = x.shape[0]
    groups, _, _, width = g0.shape
    heads = width // HEAD_DIM
    return pl.pallas_call(
        attention_backward,
        grid=(groups,),
        in_specs=[
            whole(n, D), group(4, D, width), whole(16, D), whole(n, D), whole(n, D),
            whole(D, n), group(n, width), group(n, width), group(width, n),
            group(heads, n, n), group(n, width), whole(D, n),
        ],
        out_specs=[group(4, D, width), whole(n, D), whole(8, D), group(8, width)],
        out_shape=[
            shaped(BF16, groups, 4, D, width), shaped(BF16, n, D), shaped(F32, 8, D),
            shaped(F32, groups, 8, width),
        ],
        scratch_shapes=[
            pltpu.VMEM((n, width), BF16), pltpu.VMEM((16, n), F32), pltpu.VMEM((width, n), F32),
            pltpu.VMEM((n, width), BF16), pltpu.VMEM((n, width), BF16),
            pltpu.VMEM((n, width), BF16), pltpu.VMEM((n, D), F32),
        ],
        compiler_params=pltpu.CompilerParams(vmem_limit_bytes=VMEM_LIMIT),
        name="attention_backward",
    )(x, g0, rows, dh1, gb, gbt, q, v, kt, p, o, a1t)


Z_DEV, Y_DEV, X_DEV, C_DEV = 4, 2, 2, 2


class Place:
    def __init__(self):
        dp, self.t = lax.axis_index("dp"), lax.axis_index("tensor")
        self.dp = dp
        self.z, self.y = dp // 2, dp % 2
        self.x, self.c = self.t // 2, self.t % 2
        self.other_y = 1 - self.y
        self.zs = [
            self.z,
            self.z + 1 - 2 * (self.z % 2),
            self.z + 2 - 4 * (self.z // 2),
            3 - self.z,
        ]
        self.ts = [
            self.t,
            self.t + 1 - 2 * (self.t % 2),
            self.t + 2 - 4 * (self.t // 2),
            3 - self.t,
        ]
        self.to_z = [dict(dp=z * 2 + self.y) for z in self.zs]
        self.to_y = dict(dp=self.z * 2 + self.other_y)
        self.to_x = dict(tensor=self.ts[2])
        self.to_core = dict(tensor=self.ts[1])

    def group(self, k):
        return lax.select(
            k == 0, self.ts[0],
            lax.select(k == 1, self.ts[1], lax.select(k == 2, self.ts[2], self.ts[3])),
        )

    def greet(self):
        barrier = pltpu.get_barrier_semaphore()
        others = self.to_z[1:] + [self.to_y, self.to_x, self.to_core]
        for device in others:
            pl.semaphore_signal(
                barrier, inc=1, device_id=device, device_id_type=pl.DeviceIdType.MESH
            )
        pl.semaphore_wait(barrier, len(others))


class Links:
    def __init__(self, send_sem, recv_sem):
        self.send_sem, self.recv_sem = send_sem, recv_sem
        self.copies = []

    def add(self, device, src, dst):
        number = len(self.copies)
        copy = pltpu.make_async_remote_copy(
            src_ref=src,
            dst_ref=dst,
            send_sem=self.send_sem.at[number],
            recv_sem=self.recv_sem.at[number],
            device_id=device,
            device_id_type=pl.DeviceIdType.MESH,
        )
        self.copies.append(copy)
        return copy

    def sent(self, *apart):
        for copy in self.copies:
            if all(copy is not other for other in apart):
                copy.wait_send()


def flat(copies):
    for item in copies:
        if isinstance(item, list):
            yield from flat(item)
        else:
            yield item


def start(*copies):
    for copy in flat(copies):
        copy.start()


def recv(*copies):
    for copy in flat(copies):
        copy.wait_recv()


class Gather:
    def __init__(self, links, place, own, full, x_first, single=True):
        every = slice(None)
        y, other = place.y, place.other_y

        def same(device, k, yy, to):
            return links.add(device, full(k, every, yy), full(to, every, yy))

        if x_first:
            self.first = [links.add(place.to_x, own, full(2, place.z, y))]
        self.z = [
            links.add(place.to_z[k], own, full(0, place.z, y)) for k in range(1, 4)
        ]
        if x_first:
            far = full(2, place.z, y)
            self.far = [links.add(place.to_z[k], far, far) for k in range(1, 4)]
            self.second = [same(place.to_y, 0, y, 0), same(place.to_y, 2, y, 2)]
            blocks = [(0, y), (2, y), (0, other), (2, other)]
        else:
            if single:
                self.first = [same(place.to_y, 0, y, 0)]
            else:
                self.first = [links.add(place.to_y, own, full(0, place.z, y))]
                for k in range(1, 4):
                    block = full(0, place.zs[k], y)
                    self.first.append(links.add(place.to_y, block, block))
            self.second = [same(place.to_x, 0, y, 2), same(place.to_x, 0, other, 2)]
            blocks = [(0, y), (0, other), (2, y), (2, other)]
        self.core = [same(place.to_core, k, yy, k + 1) for k, yy in blocks]


def fused_forward(
    tie_ref, len_ref, tokens_ref, gains_ref, bias_ref, in_ref, out_ref, expand_ref,
    project_ref,
    gq_ref, gw_ref, flat1_ref, flat2_ref, rows_ref,
    q_ref, v_ref, kt_ref, p_ref, scale_ref, o_ref, a1t_ref, h1_ref, a2_ref, a2t_ref,
    own0_ref, ownw_ref, own1_ref, own2_ref, square_ref, vec_ref,
    all0_ref, allw_ref, w1_ref, w2_ref, vecs_ref, bqv_ref, x_ref, a1_ref, k_ref, qa_ref, vt_ref,
    ot_ref,
    send_sem, recv_sem, local_sem,
):
    t = pl.program_id(0)
    n, _ = x_ref.shape
    width = allw_ref.shape[-1]
    heads = width // HEAD_DIM
    step = 256
    place = Place()
    length = len_ref[place.t]
    links = Links(send_sem, recv_sem)
    z, y, x, c = place.z, place.y, place.x, place.c
    vec_z = [
        links.add(place.to_z[k], vec_ref, vecs_ref.at[z, y, x, c]) for k in range(1, 4)
    ]
    vec_y = links.add(place.to_y, vecs_ref.at[:, y, x, c], vecs_ref.at[:, y, x, c])
    vec_x = links.add(place.to_x, vecs_ref.at[:, :, x, c], vecs_ref.at[:, :, x, c])
    vec_core = links.add(place.to_core, vecs_ref.at[:, :, :, c], vecs_ref.at[:, :, :, c])
    seg0 = Gather(
        links, place, own0_ref, lambda k, z, y: all0_ref.at[k, z, y], False, False
    )
    segw = Gather(links, place, ownw_ref, lambda k, z, y: allw_ref.at[k, z, y], False)
    seg1 = Gather(links, place, own1_ref, lambda k, z, y: w1_ref.at[k, z, y], False)
    seg2 = Gather(links, place, own2_ref, lambda k, z, y: w2_ref.at[k, z, y], True)
    flush = [
        pltpu.make_async_copy(w1_ref, flat1_ref, local_sem.at[0]),
        pltpu.make_async_copy(w2_ref, flat2_ref, local_sem.at[1]),
    ]
    fetch = pltpu.make_async_copy(tokens_ref.at[place.t], x_ref, local_sem.at[2])

    def pass_on(seg, stage):
        if stage == 0:
            recv(seg.z)
            start(seg.first, seg.second[0], seg.core[0])
        elif stage == 1:
            recv(seg.first)
            start(seg.second[1], seg.core[1])
        else:
            recv(seg.second[stage - 2])
            start(seg.core[stage])

    @pl.when(t == 0)
    def _():
        s0, s1, s2, s3 = tie_ref[0], tie_ref[1], tie_ref[2], tie_ref[3]
        fetch.start()
        square_ref[...] = jnp.zeros_like(square_ref)
        gain = gains_ref.shape[-1]
        square_ref[0:1, :gain] = gains_ref[s0].astype(F32)[0:1]
        square_ref[1:2, :gain] = gains_ref[s2].astype(F32)[1:2]
        kinds = [s0, s0, s0, s1, s2, s3, s2, s2, s2, s2]
        for i, source in enumerate(kinds):
            wide = bias_ref[i].astype(F32)
            here = lax.broadcasted_iota(jnp.int32, wide.shape, 0) == source
            square_ref[2 + i : 3 + i, :gain] = jnp.sum(
                jnp.where(here, wide, 0.0), 0, keepdims=True
            )
        vec_ref[...] = square_ref[...].T[:gain]
        for j in range(3):
            own0_ref[:, j * width : (j + 1) * width] = in_ref[s0, j]
        place.greet()
        start(vec_z, seg0.z[1], seg0.z[2], seg0.z[0], seg0.first[0])
        vecs_ref[z, y, x, c] = vec_ref[...]
        all0_ref[0, z, y] = own0_ref[...]
        ownw_ref[...] = out_ref[s1].T
        allw_ref[0, z, y] = ownw_ref[...]
        own1_ref[...] = expand_ref[s2]
        own2_ref[...] = project_ref[s3]
        w1_ref[0, z, y] = own1_ref[...]
        w2_ref[0, z, y] = own2_ref[...]
        recv(vec_z)
        start(vec_y)
        recv(seg0.z[0])
        start(seg0.first[1])
        recv(vec_y)
        start(vec_x)
        recv(vec_x)
        start(vec_core)
        recv(seg0.z[1])
        start(seg0.first[2])
        start(segw.z, seg2.first, seg1.z, seg2.z)
        recv(vec_core)
        vecs = vecs_ref[...].reshape(D, vecs_ref.shape[-1]).T[:16]
        rows_ref[...] = vecs
        for k in range(4):
            part = slice(k * width, (k + 1) * width)
            bqv_ref[k, 0:1, :width] = vecs[3:4, part]
            bqv_ref[k, 0:1, width : 2 * width] = jnp.zeros((1, width), F32)
            bqv_ref[k, 0:1, 2 * width :] = vecs[4:5, part]
        fetch.wait()

        @pl.loop(0, n // step)
        def _(b):
            rows = pl.ds(pl.multiple_of(b * step, step), step)
            wide = x_ref[rows, :].astype(F32)
            xhat, _ = norm_parts(wide)
            a1 = (xhat * rows_ref[0:1, :] + rows_ref[2:3, :]).astype(BF16)
            a1_ref[rows, :] = a1
            a1t_ref[:, rows] = a1.T
            h1_ref[rows, :] = wide + rows_ref[5:6, :]

        recv(seg0.z[2])
        start(seg0.first[3], seg0.second[0], seg0.core[0])
        recv(seg0.first)
        start(seg0.second[1], seg0.core[1])
        pass_on(segw, 0)

    @pl.when(t == 1)
    def _():
        recv(seg0.core[0], seg0.core[1])

    @pl.when(t == 2)
    def _():
        recv(seg2.z)
        start(seg2.second[0], seg2.core[0])
        pass_on(segw, 3)

    @pl.when(t == 3)
    def _():
        recv(seg0.core[2], seg0.core[3])
        pass_on(seg1, 2)
        recv(seg2.far)
        start(seg2.second[1], seg2.core[1])
        pass_on(seg2, 2)

    gq_ref[0] = all0_ref[t].reshape(gq_ref.shape[1:])
    mine = place.group(t)
    qkv = dot_nn(a1_ref[...], gq_ref[0]) + bqv_ref[mine, 0:1, :]
    q = qkv[:, :width].astype(BF16)
    k = qkv[:, width : 2 * width].astype(BF16)
    v = qkv[:, 2 * width :].astype(BF16)
    q = q * jnp.asarray(HEAD_DIM ** -0.5, BF16)
    q_ref[0] = q
    kt_ref[0] = k.T
    v_ref[0] = v
    vt_ref[...] = v.T
    spare = k_ref.shape[1] - width
    extra = lax.broadcasted_iota(jnp.int32, (n, spare), 1) == 0
    dead = lax.broadcasted_iota(jnp.int32, (n, spare), 0) >= length
    k_ref[:, :width] = k
    k_ref[:, width:] = jnp.where(extra & dead, MASKED, 0.0).astype(BF16)
    qa_ref[:, :width] = q
    qa_ref[:, width:] = jnp.where(extra, 1.0, 0.0).astype(BF16)

    units = [(h, b) for h in range(heads) for b in range(n // step)]

    def scores(h, b):
        first, last = b * step, (b + 1) * step
        q = qa_ref[first:last, :]
        lane = lax.broadcasted_iota(jnp.int32, (1, q.shape[1]), 1)
        keep = head_mask((1, q.shape[1]), h) | (lane >= width)
        return dot_nt(k_ref[:last, :], jnp.where(keep, q, jnp.zeros((), BF16)))

    def attend(h, b, s):
        first, last = b * step, (b + 1) * step
        key = lax.broadcasted_iota(jnp.int32, (step, step), 0)
        query = lax.broadcasted_iota(jnp.int32, (step, step), 1)
        near = jnp.where(key <= query, s[first:], MASKED)
        head = slice(h * HEAD_DIM, (h + 1) * HEAD_DIM)
        top = jnp.max(near, 0, keepdims=True)
        if b:
            far = s[:first]
            top = jnp.maximum(top, jnp.max(far, 0, keepdims=True))
        e_near = jnp.exp(near - top)
        total = jnp.sum(e_near, 0, keepdims=True)
        e_near = e_near.astype(BF16)
        p_ref[0, h, first:last, first:last] = e_near
        o = dot_nn(vt_ref[head, first:last], e_near)
        if b:
            e_far = jnp.exp(far - top)
            total += jnp.sum(e_far, 0, keepdims=True)
            e_far = e_far.astype(BF16)
            p_ref[0, h, :first, first:last] = e_far
            o += dot_nn(vt_ref[head, :first], e_far)
        scale = 1.0 / total
        scale_ref[0, h : h + 1, first:last] = scale
        ot_ref[head, first:last] = (o * scale).astype(BF16)

    scale_ref[0, heads:, :] = jnp.zeros((scale_ref.shape[1] - heads, n), F32)
    s = scores(*units[0])
    for i, unit in enumerate(units):
        ahead = scores(*units[i + 1]) if i + 1 < len(units) else None
        attend(*unit, s)
        s = ahead

    @pl.when(t == 0)
    def _():
        pass_on(seg0, 2)
        pass_on(segw, 1)
        pass_on(seg1, 0)

    @pl.when(t == 1)
    def _():
        pass_on(seg0, 3)
        recv(seg2.first)
        start(seg2.far)
        pass_on(seg1, 1)
        recv(segw.core[0], segw.core[1])

    @pl.when(t == 2)
    def _():
        pass_on(segw, 2)

    @pl.when(t == 3)
    def _():
        recv(segw.core[2], segw.core[3])

    gw_ref[0] = allw_ref[t].reshape(gw_ref.shape[1:])
    o = ot_ref[...].T
    o_ref[0] = o
    h1_ref[...] += dot_nt(o, gw_ref[0])

    @pl.when(t == 3)
    def _():
        pass_on(seg1, 3)

        @pl.loop(0, n // step)
        def _(b):
            rows = pl.ds(pl.multiple_of(b * step, step), step)
            h1 = h1_ref[rows, :]
            xhat, _ = norm_parts(h1)
            a2 = (xhat * rows_ref[1:2, :] + rows_ref[6:7, :]).astype(BF16)
            a2_ref[rows, :] = a2
            a2t_ref[:, rows] = a2.T

        pass_on(seg2, 3)
        recv(seg1.core)
        flush[0].start()
        recv(seg2.core)
        flush[1].start()
        links.sent()
        for copy in flush:
            copy.wait()


N_GATHER = 6 + 13 + 10 + 10 + 13
VMEM_WHOLE = pl.BlockSpec(memory_space=pltpu.VMEM)
ANY_WHOLE = pl.BlockSpec(memory_space=pl.ANY)


def run_fused_forward(tie, lengths, tokens, gains, biases, w_in, w_out, w_expand, w_project):
    groups, n, _ = tokens.shape
    depth, width = w_in.shape[-2:]
    heads = width // HEAD_DIM
    hidden = w_expand.shape[-1]
    w_project = w_project.transpose(0, 2, 1)
    biases = biases.transpose(1, 0, 2)
    own = gains.shape[-1]
    return pl.pallas_call(
        fused_forward,
        grid=(groups,),
        in_specs=[SMEM_WHOLE, SMEM_WHOLE, ANY_WHOLE] + [VMEM_WHOLE] * 6,
        out_specs=[
            group(D, 3 * width), group(D, width), ANY_WHOLE, ANY_WHOLE, VMEM_WHOLE,
            group(n, width), group(n, width), group(width, n), group(heads, n, n),
            group(8, n), group(n, width), VMEM_WHOLE, VMEM_WHOLE, VMEM_WHOLE, VMEM_WHOLE,
        ],
        out_shape=[
            shaped(BF16, groups, D, 3 * width), shaped(BF16, groups, D, width),
            shaped(BF16, groups, Z_DEV, Y_DEV, depth, hidden),
            shaped(BF16, groups, Z_DEV, Y_DEV, depth, hidden),
            shaped(F32, 16, D),
            shaped(BF16, groups, n, width), shaped(BF16, groups, n, width),
            shaped(BF16, groups, width, n), shaped(BF16, groups, heads, n, n),
            shaped(F32, groups, 8, n), shaped(BF16, groups, n, width), shaped(BF16, D, n), shaped(F32, n, D),
            shaped(BF16, n, D), shaped(BF16, D, n),
        ],
        scratch_shapes=[
            pltpu.VMEM((depth, 3 * width), BF16), pltpu.VMEM((depth, width), BF16),
            pltpu.VMEM((depth, hidden), BF16), pltpu.VMEM((depth, hidden), BF16),
            pltpu.VMEM((128, 128), F32), pltpu.VMEM((own, 128), F32),
            pltpu.VMEM((groups, Z_DEV, Y_DEV, depth, 3 * width), BF16),
            pltpu.VMEM((groups, Z_DEV, Y_DEV, depth, width), BF16),
            pltpu.VMEM((groups, Z_DEV, Y_DEV, depth, hidden), BF16),
            pltpu.VMEM((groups, Z_DEV, Y_DEV, depth, hidden), BF16),
            pltpu.VMEM((Z_DEV, Y_DEV, X_DEV, C_DEV, own, 128), F32),
            pltpu.VMEM((groups, 8, 3 * width), F32),
            pltpu.VMEM((n, D), BF16), pltpu.VMEM((n, D), BF16), pltpu.VMEM((n, 256), BF16),
            pltpu.VMEM((n, 256), BF16), pltpu.VMEM((width, n), BF16),
            pltpu.VMEM((width, n), BF16),
            pltpu.SemaphoreType.DMA((N_GATHER,)), pltpu.SemaphoreType.DMA((N_GATHER,)),
            pltpu.SemaphoreType.DMA((3,)),
        ],
        compiler_params=pltpu.CompilerParams(
            vmem_limit_bytes=VMEM_LIMIT, collective_id=0, has_side_effects=True
        ),
        name="fused_forward",
    )(tie, lengths, tokens, gains, biases, w_in, w_out, w_expand, w_project)


class Result:
    def __init__(self, links, place, own_ref, passing_ref, out_ref, step, sem):
        count = own_ref.shape[0] // step
        self.own_ref, self.passing_ref, self.out_ref, self.sem = own_ref, passing_ref, out_ref, sem
        self.place = place
        self.x, self.core, self.far = [], [], []
        for i in range(count):
            rows = pl.ds(i * step, step)
            mine, theirs = out_ref.at[place.t, rows], out_ref.at[place.ts[2], rows]
            self.x.append(links.add(place.to_x, own_ref.at[rows], passing_ref.at[rows]))
            self.core.append(links.add(place.to_core, own_ref.at[rows], mine))
            self.far.append(links.add(place.to_core, passing_ref.at[rows], theirs))

    def send(self, i):
        start(self.x[i], self.core[i])

    def pass_on(self, i):
        recv(self.x[i])
        start(self.far[i])

    def finish(self):
        for ref, where in [
            (self.own_ref, self.place.t), (self.passing_ref, self.place.ts[2])
        ]:
            copy = pltpu.make_async_copy(ref, self.out_ref.at[where], self.sem)
            copy.start()
            copy.wait()
        recv(self.core, self.far)


def group_order(i):
    return (1 + 2 * i) % 4 - i // 2


def fused_feed_forward(
    len_ref, cot_ref, a2_ref, a2t_ref, h1_ref, w1_ref, w2_ref, rows_ref,
    out_ref, rest_ref, d1_ref, d2_ref, dh1_ref, gb_ref, gbt_ref, sums_ref,
    gf_ref, gft_ref, feed_ref, h_ref, slope_ref,
    land1_ref, stage2_ref, land2_ref, work2_ref, cross2_ref, own_ref, passing_ref, c_ref,
    send_sem, recv_sem, local_sem,
):
    t = pl.program_id(0)
    n = c_ref.shape[0]
    da2_ref, stage1_ref = feed_ref, stage2_ref
    step = 256
    big = 512
    depth = stage2_ref.shape[-2]
    place = Place()
    length = len_ref[place.t]
    links = Links(send_sem, recv_sem)
    y, other = place.y, place.other_y
    core2 = [links.add(place.to_core, stage2_ref.at[i], land2_ref.at[i]) for i in range(2)]
    core1 = [links.add(place.to_core, stage1_ref.at[i], land1_ref.at[i]) for i in range(2)]
    cross2 = [
        links.add(place.to_y, work2_ref.at[i, :, other], cross2_ref.at[i]) for i in range(2)
    ]
    half = n // 2
    out = Result(links, place, own_ref, passing_ref, out_ref, half // 2, local_sem.at[1])
    fetch = pltpu.make_async_copy(cot_ref.at[place.t], c_ref, local_sem.at[0])
    k = group_order(t % 4)
    mine = place.group(k)

    def weight_grad(left_ref, right):
        value = dot_nn(left_ref[...], right)
        return value.reshape(Z_DEV, Y_DEV, depth, value.shape[-1])

    @pl.when(t == 0)
    def _():
        fetch.start()
        place.greet()
        sums_ref[...] = jnp.zeros_like(sums_ref)
        fetch.wait()

        @pl.loop(0, n // step)
        def _(b):
            rows = pl.ds(pl.multiple_of(b * step, step), step)
            at = b * step + lax.broadcasted_iota(jnp.int32, (step, 1), 0)
            live = (at < length).astype(F32)
            g = (c_ref[rows, :].astype(F32) * live).astype(BF16)
            gf_ref[rows, :] = g
            gft_ref[:, rows] = g.T
            sums_ref[7:8, :] += jnp.sum(g.astype(F32), 0, keepdims=True)

    @pl.when(t < 4)
    def _():
        bias = rows_ref[pl.ds(8 + mine, 1), :]

        @pl.loop(0, n // big)
        def _(b):
            rows = pl.ds(pl.multiple_of(b * big, big), big)
            f = dot_nn(a2_ref[rows, :], w1_ref[0]) + bias
            f2 = f * f
            th = jnp.tanh(f * (SQRT_2_PI + (SQRT_2_PI * 0.044715) * f2))
            half = 0.5 + 0.5 * th
            h = (f * half).astype(BF16)
            slope = half + f * (0.5 - 0.5 * th * th) * (
                SQRT_2_PI + (3 * SQRT_2_PI * 0.044715) * f2
            )
            h_ref[k, rows, :] = h
            slope_ref[k, rows, :] = slope.astype(BF16)
            feed = dot_nt(h, w2_ref[0])

            @pl.when(t == 0)
            def _():
                feed_ref[rows, :] = feed

            @pl.when(t > 0)
            def _():
                feed_ref[rows, :] += feed

    @pl.when(t < 2)
    def _():
        stage2_ref[t] = weight_grad(gft_ref, h_ref[k]).astype(BF16)
        for i in range(2):
            @pl.when(t == i)
            def _():
                start(core2[i])

    @pl.when(t == 3)
    def _():
        @pl.loop(0, n // step)
        def _(b):
            rows = pl.ds(pl.multiple_of(b * step, step), step)
            at = b * step + lax.broadcasted_iota(jnp.int32, (step, 1), 0)
            live = (at < length).astype(F32)
            value = (
                live * (h1_ref[rows, :] + (feed_ref[rows, :] + rows_ref[7:8, :]))
            ).astype(BF16)

            @pl.when(b < half // step)
            def _():
                own_ref[rows, :] = value

            @pl.when(b >= half // step)
            def _():
                rest_ref[pl.ds(pl.multiple_of(b * step - half, step), step), :] = value

        out.send(0)
        out.send(1)

    @pl.when((t == 4) | (t == 5))
    def _():
        for i in range(2):
            @pl.when(t == 4 + i)
            def _():
                recv(core2[i])

        value = weight_grad(gft_ref, h_ref[2 * (t - 4)])
        work2_ref[t - 4] = (value + land2_ref[t - 4].astype(F32)).astype(BF16)
        for i in range(2):
            @pl.when(t == 4 + i)
            def _():
                start(cross2[i])

    @pl.when(t >= 4)
    def _():
        @pl.loop(0, n // big)
        def _(b):
            rows = pl.ds(pl.multiple_of(b * big, big), big)
            dh = dot_nn(gf_ref[rows, :], w2_ref[0])
            df = (dh * slope_ref[k, rows, :].astype(F32)).astype(BF16)
            slope_ref[k, rows, :] = df
            sums_ref[pl.ds(8 + mine, 1), :] += jnp.sum(df.astype(F32), 0, keepdims=True)
            da2 = dot_nt(df, w1_ref[0])

            @pl.when(t == 4)
            def _():
                da2_ref[rows, :] = da2

            @pl.when(t > 4)
            def _():
                da2_ref[rows, :] += da2

    @pl.when((t == 4) | (t == 5))
    def _():
        for i in range(2):
            @pl.when(t == 4 + i)
            def _():
                core2[i].wait_send()

        stage1_ref[t - 4] = weight_grad(a2t_ref, slope_ref[k]).astype(BF16)
        for i in range(2):
            @pl.when(t == 4 + i)
            def _():
                start(core1[i])

    @pl.when(t >= 6)
    def _():
        for i in range(2):
            @pl.when(t == 6 + i)
            def _():
                recv(core1[i])
                out.pass_on(i)

        value = weight_grad(a2t_ref, slope_ref[k])
        d1_ref[t - 6] = (value + land1_ref[t - 6].astype(F32)).astype(BF16)

    @pl.when(t == 7)
    def _():
        @pl.loop(0, n // step)
        def _(b):
            rows = pl.ds(pl.multiple_of(b * step, step), step)
            at = b * step + lax.broadcasted_iota(jnp.int32, (step, 1), 0)
            live = (at < length).astype(F32)
            xhat, r = norm_parts(h1_ref[rows, :])
            da2 = da2_ref[rows, :]
            sums_ref[1:2, :] += jnp.sum(da2 * xhat, 0, keepdims=True)
            sums_ref[6:7, :] += jnp.sum(da2, 0, keepdims=True)
            dg = da2 * rows_ref[1:2, :]
            dv = r * (
                dg
                - jnp.mean(dg, -1, keepdims=True)
                - xhat * jnp.mean(dg * xhat, -1, keepdims=True)
            )
            dh1 = live * c_ref[rows, :].astype(F32) + dv
            dh1_ref[rows, :] = dh1
            gb = dh1.astype(BF16)
            gb_ref[rows, :] = gb
            gbt_ref[:, rows] = gb.T
            sums_ref[5:6, :] += jnp.sum(gb.astype(F32), 0, keepdims=True)

        recv(cross2[0], cross2[1])

        @pl.loop(0, Z_DEV)
        def _(z):
            for i in range(2):
                d2_ref[i, z] = (
                    work2_ref[i, z, y].astype(F32) + cross2_ref[i, z].astype(F32)
                ).astype(BF16)

        out.finish()
        links.sent(*core2)


def run_fused_feed_forward(lengths, cot, a2, a2t, h1, g1, g2, rows):
    n = cot.shape[1]
    groups, hidden = g1.shape[0], g1.shape[-1]
    depth = D // (Z_DEV * Y_DEV)
    halves = (2, Z_DEV, Y_DEV, depth, hidden)
    weight = pl.BlockSpec((1, D, hidden), lambda t: (group_order(t % 4), 0, 0))
    return pl.pallas_call(
        fused_feed_forward,
        grid=(2 * groups,),
        in_specs=[SMEM_WHOLE, ANY_WHOLE] + [VMEM_WHOLE] * 3 + [weight, weight, VMEM_WHOLE],
        out_specs=[ANY_WHOLE] + [VMEM_WHOLE] * 7,
        out_shape=[
            shaped(BF16, groups, n // 2, D), shaped(BF16, n // 2, D), shaped(BF16, *halves),
            shaped(BF16, 2, Z_DEV, depth, hidden), shaped(F32, n, D), shaped(BF16, n, D),
            shaped(BF16, D, n), shaped(F32, 16, D),
        ],
        scratch_shapes=[
            pltpu.VMEM((n, D), BF16), pltpu.VMEM((D, n), BF16), pltpu.VMEM((n, D), F32),
            pltpu.VMEM((groups, n, hidden), BF16),
            pltpu.VMEM((groups, n, hidden), BF16),
            pltpu.VMEM(halves, BF16), pltpu.VMEM(halves, BF16), pltpu.VMEM(halves, BF16),
            pltpu.VMEM(halves, BF16),
            pltpu.VMEM((2, Z_DEV, depth, hidden), BF16), pltpu.VMEM((n // 2, D), BF16),
            pltpu.VMEM((n // 2, D), BF16), pltpu.VMEM((n, D), BF16),
            pltpu.SemaphoreType.DMA((12,)), pltpu.SemaphoreType.DMA((12,)),
            pltpu.SemaphoreType.DMA((3,)),
        ],
        compiler_params=pltpu.CompilerParams(
            vmem_limit_bytes=VMEM_LIMIT, collective_id=1, has_side_effects=True
        ),
        name="fused_feed_forward",
    )(lengths, cot, a2, a2t, h1, g1, g2, rows)


class Reduce:
    def __init__(self, links, place, work, acc, cross_ref, far_ref, last_ref, side_ref):
        self.place, self.work, self.acc = place, work, acc
        self.cross_ref, self.far_ref = cross_ref, far_ref
        self.last_ref, self.side_ref = last_ref, side_ref
        zs = place.zs
        self.y = []
        if cross_ref is not None:
            self.y = [
                [
                    links.add(
                        place.to_y, work(s, zs[j], place.other_y), cross_ref.at[s, zs[j]]
                    )
                    for j in (1, 2, 3, 0)
                ]
                for s in range(2)
            ]
        self.z = [
            [
                links.add(place.to_z[j], acc(s, zs[j]), far_ref.at[s, j - 1])
                for j in range(1, 4)
            ]
            for s in range(2)
        ]
        self.x = links.add(place.to_x, last_ref, side_ref)

    def fold_y(self, s):
        for i, j in enumerate((1, 2, 3, 0)):
            z = self.place.zs[j]
            recv(self.y[s][i])
            value = self.work(s, z, self.place.y)[...].astype(F32)
            self.acc(s, z)[...] = (value + self.cross_ref[s, z].astype(F32)).astype(BF16)
            if j:
                start(self.z[s][j - 1])

    def own(self, s):
        recv(self.z[s])
        far = self.far_ref
        return self.acc(s, self.place.z)[...].astype(F32) + (
            far[s, 0].astype(F32) + far[s, 1].astype(F32) + far[s, 2].astype(F32)
        )

    def send_x(self):
        self.last_ref[...] = self.own(1).astype(BF16)
        start(self.x)

    def total(self):
        value = self.own(0)
        recv(self.x)
        return value + self.side_ref[...].astype(F32)


def fused_backward(
    tokens_ref, gq_ref, gw_ref, rows_ref, dh1_ref, gb_ref, gbt_ref, q_ref, v_ref, kt_ref,
    p_ref, scale_ref, o_ref, a1t_ref, rest_ref, d1_ref, d2_ref, early_ref,
    out_ref, later_ref, part0_ref, partw_ref, part1_ref, part2_ref, total_ref,
    do_ref, delta_ref, dqt_ref, dqkv_ref, da1_ref, own_ref, passing_ref, passrest_ref, bqv_ref,
    work1_ref, cross1_ref, far1_ref, last1_ref, side1_ref,
    far2_ref, last2_ref, side2_ref,
    stagew_ref, landw_ref, workw_ref, crossw_ref, farw_ref, lastw_ref, sidew_ref,
    stage0_ref, land0_ref, work0_ref, cross0_ref, far0_ref, last0_ref, side0_ref,
    sums_ref, sumland_ref,
    send_sem, recv_sem, local_sem,
):
    t = pl.program_id(0)
    n = own_ref.shape[0]
    width = gw_ref.shape[-1]
    depth = part0_ref.shape[0]
    heads = width // HEAD_DIM
    step = n // 4
    place = Place()
    y = place.y
    links = Links(send_sem, recv_sem)
    k, b = group_and_block(t)
    mine = place.group(k)
    out = Result(links, place, own_ref, passing_ref, out_ref, step, local_sem.at[0])
    rest = Result(links, place, rest_ref, passrest_ref, later_ref, step, local_sem.at[1])
    fetch = pltpu.make_async_copy(tokens_ref.at[place.t], own_ref, local_sem.at[2])
    corew = [links.add(place.to_core, stagew_ref.at[i], landw_ref.at[i]) for i in range(2)]
    core0 = [links.add(place.to_core, stage0_ref.at[i], land0_ref.at[i]) for i in range(2)]
    seg1 = Reduce(
        links, place, lambda s, z, y: d1_ref.at[s, z, y], lambda s, z: work1_ref.at[s, z],
        cross1_ref, far1_ref, last1_ref, side1_ref,
    )
    seg2 = Reduce(
        links, place, None, lambda s, z: d2_ref.at[s, z], None, far2_ref, last2_ref, side2_ref
    )
    segw = Reduce(
        links, place, lambda s, z, y: workw_ref.at[s, z, y],
        lambda s, z: workw_ref.at[s, z, y],
        crossw_ref, farw_ref, lastw_ref, sidew_ref,
    )
    seg0 = Reduce(
        links, place, lambda s, z, y: work0_ref.at[s, z, y],
        lambda s, z: work0_ref.at[s, z, y],
        cross0_ref, far0_ref, last0_ref, side0_ref,
    )
    sum_core, sum_y, *sum_z, sum_x = [
        links.add(to, sums_ref.at[i], sumland_ref.at[j])
        for j, (i, to) in enumerate(
            zip([0, 1, 2, 2, 2, 3], [place.to_core, place.to_y] + place.to_z[1:] + [place.to_x])
        )
    ]

    def when(now):
        return pl.when(t == now)

    @when(0)
    def _():
        fetch.start()
        place.greet()
        rest.send(0)
        rest.send(1)
        start(seg1.y[1], seg1.y[0], seg2.z[1], seg2.z[0])
        bqv_ref[...] = jnp.zeros_like(bqv_ref)
        sums_ref[0] = early_ref[...]
        da1_ref[...] = jnp.zeros_like(da1_ref)
        fetch.wait()

    @when(2)
    def _():
        rest.pass_on(0)

    @when(3)
    def _():
        seg1.fold_y(1)

    @when(4)
    def _():
        rest.pass_on(1)
        recv(corew)
        for i in range(2):
            @pl.loop(0, Z_DEV)
            def _(z):
                workw_ref[i, z] = (
                    workw_ref[i, z].astype(F32) + landw_ref[i, z].astype(F32)
                ).astype(BF16)

        start(segw.y[1], segw.y[0])

    @when(5)
    def _():
        seg1.fold_y(0)

    @when(6)
    def _():
        seg2.send_x()

    @when(7)
    def _():
        out.pass_on(0)

    @when(9)
    def _():
        segw.fold_y(1)
        segw.fold_y(0)

    @when(11)
    def _():
        seg1.send_x()
        out.pass_on(1)

    @pl.when(t < 4)
    def _():
        pick = (
            lax.broadcasted_iota(jnp.int32, (16, width), 1) // HEAD_DIM
            == lax.broadcasted_iota(jnp.int32, (16, width), 0)
        ).astype(BF16)

        @pl.loop(0, n // step)
        def _(i):
            rows = pl.ds(pl.multiple_of(i * step, step), step)
            columns = scale_ref[0, :, rows].T
            lane = lax.broadcasted_iota(jnp.int32, (step, width), 1)
            scale = columns[:, heads - 1 : heads]
            for h in reversed(range(heads - 1)):
                scale = jnp.where(lane < (h + 1) * HEAD_DIM, columns[:, h : h + 1], scale)
            do = (dot_nn(gb_ref[rows, :], gw_ref[0]) * scale).astype(BF16)
            do_ref[k, rows, :] = do
            prod = do.astype(F32) * o_ref[0, rows, :].astype(F32)
            high = prod.astype(BF16)
            low = (prod - high.astype(F32)).astype(BF16)
            delta_ref[k, :, rows] = dot_nt(pick, high) + dot_nt(pick, low)

        dqt_ref[k] = jnp.zeros(dqt_ref.shape[1:], F32)
        value = dot_nn(gbt_ref[...], o_ref[0]).reshape(Z_DEV, Y_DEV, depth, width)
        for i in range(2):
            @when(2 * i)
            def _():
                stagew_ref[i] = value.astype(BF16)
                start(corew[i])

            @when(2 * i + 1)
            def _():
                workw_ref[i] = value.astype(BF16)

    for bb in range(4):
        @pl.when(b == bb)
        def _():
            first, last = bb * step, (bb + 1) * step
            do = do_ref[k, first:, :]
            q = q_ref[0, first:, :]
            v = v_ref[0, first:last, :]
            lane = lax.broadcasted_iota(jnp.int32, (1, width), 1)
            dk, dv = None, None
            for h in range(heads):
                lanes = head_mask((1, width), h)
                zero = jnp.zeros((), BF16)
                p = p_ref[0, h, :, first:]
                dp = dot_nt(jnp.where(lanes, v, zero), do)
                ds = (p.astype(F32) * (dp - delta_ref[k, h : h + 1, first:])).astype(BF16)
                part = dot_nn(p, do)
                dv = part if dv is None else jnp.where(lane < h * HEAD_DIM, dv, part)
                part = dot_nn(ds, q)
                dk = part if dk is None else jnp.where(lane < h * HEAD_DIM, dk, part)
                head = slice(h * HEAD_DIM, (h + 1) * HEAD_DIM)
                dqt_ref[k, head, first:] += dot_nn(kt_ref[0, head, first:last], ds)
            dk = dk.astype(BF16)
            dv = dv.astype(BF16)
            dq = (dqt_ref[k, :, first:last] * HEAD_DIM ** -0.5).astype(BF16).T
            dqkv_ref[k, first:last, :width] = dq
            dqkv_ref[k, first:last, width : 2 * width] = dk
            dqkv_ref[k, first:last, 2 * width :] = dv
            bqv_ref[mine, 0:1, :] += jnp.sum(dq.astype(F32), 0, keepdims=True)
            bqv_ref[mine, 1:2, :] += jnp.sum(dv.astype(F32), 0, keepdims=True)
            da1_ref[first:last, :] += dot_nt(dqkv_ref[k, first:last, :], gq_ref[0])

    @pl.when((t == 3) | (t == 7) | (t > 13))
    def _():
        rows = pl.ds(pl.multiple_of(b * step, step), step)
        xhat, r = norm_parts(own_ref[rows, :].astype(F32))
        da1 = da1_ref[rows, :]
        sums_ref[0, 0:1, :] += jnp.sum(da1 * xhat, 0, keepdims=True)
        sums_ref[0, 2:3, :] += jnp.sum(da1, 0, keepdims=True)
        dg = da1 * rows_ref[0:1, :]
        dv = r * (
            dg
            - jnp.mean(dg, -1, keepdims=True)
            - xhat * jnp.mean(dg * xhat, -1, keepdims=True)
        )
        own_ref[rows, :] = (dh1_ref[rows, :] + dv).astype(BF16)
        for i in range(4):
            @pl.when(b == i)
            def _():
                out.send(i)

    @pl.when((t > 7) & (t % 2 == 1))
    def _():
        value = dot_nn(a1t_ref[...], dqkv_ref[k]).reshape(Z_DEV, Y_DEV, depth, 3 * width)
        for i in range(2):
            @when(9 + 4 * i)
            def _():
                stage0_ref[i] = value.astype(BF16)
                start(core0[i])

            @when(11 + 4 * i)
            def _():
                recv(core0[i])
                work0_ref[i] = (value + land0_ref[i].astype(F32)).astype(BF16)
                start(seg0.y[i])

    @when(15)
    def _():
        for s in range(4):
            sums_ref[0, 3:5, s * width : (s + 1) * width] = bqv_ref[s, 0:2, :]
        start(sum_core)
        segw.send_x()
        part2_ref[...] = seg2.total()
        seg0.fold_y(0)
        recv(sum_core)
        sums_ref[1] = sums_ref[0] + sumland_ref[0]
        start(sum_y)
        part1_ref[...] = seg1.total()
        partw_ref[...] = segw.total()
        recv(sum_y)
        sums_ref[2] = sums_ref[1] + sumland_ref[1]
        start(sum_z)
        seg0.fold_y(1)
        recv(sum_z)
        sums_ref[3] = (sums_ref[2] + sumland_ref[2]) + (sumland_ref[3] + sumland_ref[4])
        start(sum_x)
        seg0.send_x()
        out.pass_on(2)
        out.pass_on(3)
        recv(sum_x)
        total_ref[...] = sums_ref[3] + sumland_ref[5]
        part0_ref[...] = seg0.total()
        rest.finish()
        out.finish()
        links.sent()


def group_and_block(t):
    early = t < 8
    later = jnp.maximum(t - 8, 0)
    i = jnp.where(early, t % 4, later // 2)
    return i + 1 - 2 * (i % 2), jnp.where(early, t // 4, 2 + later % 2)


def run_fused_backward(
    tokens, gq, gw, rows, dh1, gb, gbt, q, v, kt, p, scale, o, a1t, rest, d1, d2, early
):
    groups, n, _ = tokens.shape
    width = gw.shape[-1]
    heads = width // HEAD_DIM
    hidden = d1.shape[-1]
    depth = D // (Z_DEV * Y_DEV)
    step = n // 4

    def by_group(*shape):
        return pl.BlockSpec(
            (1,) + shape, lambda t: (group_and_block(t)[0],) + (0,) * len(shape)
        )

    p_spec = pl.BlockSpec(
        (1, heads, step, n),
        lambda t: (group_and_block(t)[0], 0, group_and_block(t)[1], 0),
    )

    def early_group(*shape):
        return pl.BlockSpec(
            (1,) + shape, lambda t: (group_and_block(jnp.minimum(t, 3))[0],) + (0,) * len(shape)
        )

    copies = 12 + 6 + 4 + 3 * 15 + 7 + 6

    def landing(lanes):
        return [
            pltpu.VMEM((2, Z_DEV, depth, lanes), BF16),
            pltpu.VMEM((2, 3, depth, lanes), BF16),
            pltpu.VMEM((depth, lanes), BF16), pltpu.VMEM((depth, lanes), BF16),
        ]

    def working(lanes):
        return [pltpu.VMEM((2, Z_DEV, Y_DEV, depth, lanes), BF16)] * 3

    return pl.pallas_call(
        fused_backward,
        grid=(4 * groups,),
        in_specs=[
            ANY_WHOLE, by_group(D, 3 * width), early_group(D, width), VMEM_WHOLE, VMEM_WHOLE,
            VMEM_WHOLE, VMEM_WHOLE, by_group(n, width), by_group(n, width),
            by_group(width, n), p_spec, early_group(8, n), early_group(n, width),
            VMEM_WHOLE, VMEM_WHOLE, VMEM_WHOLE, VMEM_WHOLE, VMEM_WHOLE,
        ],
        out_specs=[ANY_WHOLE] * 2 + [VMEM_WHOLE] * 5,
        out_shape=[
            shaped(BF16, groups, n, D), shaped(BF16, groups, n // 2, D),
            shaped(F32, depth, 3 * width),
            shaped(F32, depth, width), shaped(F32, depth, hidden),
            shaped(F32, depth, hidden), shaped(F32, 16, D),
        ],
        scratch_shapes=[
            pltpu.VMEM((groups, n, width), BF16),
            pltpu.VMEM((groups, 16, n), F32), pltpu.VMEM((groups, width, n), F32),
            pltpu.VMEM((groups, n, 3 * width), BF16), pltpu.VMEM((n, D), F32),
            pltpu.VMEM((n, D), BF16), pltpu.VMEM((n, D), BF16), pltpu.VMEM((n // 2, D), BF16),
            pltpu.VMEM((groups, 8, width), F32),
        ]
        + landing(hidden)[:1] + landing(hidden) + landing(hidden)[1:]
        + working(width) + landing(width)
        + working(3 * width) + landing(3 * width)
        + [
            pltpu.VMEM((4, 16, D), F32), pltpu.VMEM((6, 16, D), F32),
            pltpu.SemaphoreType.DMA((copies,)), pltpu.SemaphoreType.DMA((copies,)),
            pltpu.SemaphoreType.DMA((3,)),
        ],
        compiler_params=pltpu.CompilerParams(
            vmem_limit_bytes=VMEM_LIMIT, collective_id=2, has_side_effects=True
        ),
        name="fused_backward",
    )(tokens, gq, gw, rows, dh1, gb, gbt, q, v, kt, p, scale, o, a1t, rest, d1, d2, early)


def place_gradients(
    tie_ref, sums_ref, part0_ref, partw_ref, part1_ref, part2_ref, near_out_ref, near_rest_ref,
    near_grad_ref, far_out_ref, far_grad_ref, gains_ref, bias_ref, in_ref, out_ref, expand_ref,
    project_ref,
):
    half = near_out_ref.shape[1]
    far_out_ref[0, :half] = near_out_ref[0]
    far_out_ref[0, half:] = near_rest_ref[0]
    far_grad_ref[...] = near_grad_ref[...]
    own = gains_ref.shape[-1]
    width = partw_ref.shape[-1]

    @pl.when(pl.program_id(0) == 0)
    def _():
        first = (lax.axis_index("dp") * 4 + lax.axis_index("tensor")) * own
        feature = lax.broadcasted_iota(jnp.int32, (D, 128), 0)
        lane = lax.broadcasted_iota(jnp.int32, (D, 128), 1)
        chosen = ((feature == first + lane) & (lane < own)).astype(F32)
        sums = lax.dot_general(
            sums_ref[...], chosen, (((1,), (0,)), ((), ())),
            precision=lax.Precision.HIGHEST, preferred_element_type=F32,
        )[:, :own]
        s0, s1, s2, s3 = tie_ref[0], tie_ref[1], tie_ref[2], tie_ref[3]
        w_out = partw_ref[...].T

        def at(source, wanted, value):
            return jnp.where(source == wanted, value, jnp.zeros_like(value))

        row = lax.broadcasted_iota(jnp.int32, (NSRC, own), 0)
        for i, wanted in enumerate([s0, s0, s0, s1, s2, s3, s2, s2, s2, s2]):
            bias_ref[i] = jnp.where(row == wanted, sums[2 + i : 3 + i], 0.0)
        for s in range(NSRC):
            gains_ref[s, 0:1] = at(s, s0, sums[0:1])
            gains_ref[s, 1:2] = at(s, s2, sums[1:2])
            for j in range(3):
                in_ref[s, j] = at(s, s0, part0_ref[:, j * width : (j + 1) * width])
            out_ref[s] = at(s, s1, w_out)
            expand_ref[s] = at(s, s2, part1_ref[...])
            project_ref[s] = at(s, s3, part2_ref[...])


def run_place_gradients(tie, sums, part0, partw, part1, part2, out, rest, grad, like):
    slots, n, _ = grad.shape
    gains, biases, w_in, w_out, w_expand, w_project = [item.shape for item in like]
    shapes = [
        gains, (biases[1], biases[0], biases[2]), w_in, w_out, w_expand,
        (w_project[0], w_project[2], w_project[1]),
    ]
    out, grad, gains, biases, w_in, w_out, w_expand, w_project = pl.pallas_call(
        place_gradients,
        grid=(slots,),
        in_specs=[SMEM_WHOLE] + [VMEM_WHOLE] * 5
        + [group(n // 2, D), group(n // 2, D), group(n, D)],
        out_specs=[group(n, D), group(n, D)] + [VMEM_WHOLE] * 6,
        out_shape=[shaped(BF16, slots, n, D)] * 2 + [shaped(F32, *item) for item in shapes],
        compiler_params=pltpu.CompilerParams(vmem_limit_bytes=VMEM_LIMIT),
        name="place_gradients",
    )(tie, sums, part0, partw, part1, part2, out, rest, grad)
    biases = biases.transpose(1, 0, 2)
    return out, grad, gains, biases, w_in, w_out, w_expand, w_project.transpose(0, 2, 1)


def plain_step(
    tokens, lengths, tie_map, norm_gains, bias_rows, attention_in, attention_out,
    expand_weight, project_weight, cotangent,
):
    slot_rows = tokens.shape[0] // lengths.shape[0]
    me = lax.axis_index("tensor")
    in_local = lax.dynamic_index_in_dim(attention_in, tie_map[0], 0, keepdims=False)
    out_local = lax.dynamic_index_in_dim(attention_out, tie_map[1], 0, keepdims=False)
    expand_local = lax.dynamic_index_in_dim(expand_weight, tie_map[2], 0, keepdims=False)
    project_local = lax.dynamic_index_in_dim(project_weight, tie_map[3], 0, keepdims=False)
    local0 = jnp.concatenate([in_local, out_local.T[None]], 0)
    row_kinds = jnp.array([0, 0, 0, 1, 2, 3] + [2] * (FF // D), dtype=jnp.int32)
    gain_kinds = jnp.array([0, 2], dtype=jnp.int32)
    gain_pick = norm_gains[tie_map[gain_kinds], jnp.arange(2)]
    bias_pick = bias_rows[tie_map[row_kinds], jnp.arange(row_kinds.shape[0])]
    vectors = jnp.concatenate([gain_pick, bias_pick], 0)
    x = lax.dynamic_slice_in_dim(tokens, me * slot_rows, slot_rows, 0)
    cot = lax.dynamic_slice_in_dim(cotangent, me * slot_rows, slot_rows, 0)
    length = lax.dynamic_slice_in_dim(lengths, me, 1, 0)
    rows = lax.all_gather(vectors, ("dp", "tensor"), axis=1, tiled=True).astype(F32)
    rows = jnp.concatenate([rows, jnp.zeros((4, D), F32)], 0)

    def gathered(piece, axis):
        piece = lax.all_gather(piece, "dp", axis=axis, tiled=True)
        return lax.all_gather(piece, "tensor", axis=0)

    g0 = gathered(local0, 1)
    g1 = gathered(expand_local, 0)
    g2 = gathered(project_local.T, 0)
    groups, width = g0.shape[0], g0.shape[-1]
    bqv = rows[3:5].reshape(2, groups, width).transpose(1, 0, 2)
    q, v, kt, p, o, a1t, h1, a2, a2t = run_attention_forward(length, x, g0, rows, bqv)
    out, d1, d2, dh1, gb, gbt, sums = run_feed_forward(length, cot, a2, a2t, h1, g1, g2, rows)
    d0, xg, sums_in, sums_qv = run_attention_backward(
        x, g0, rows, dh1, gb, gbt, q, v, kt, p, o, a1t
    )
    layer_out = lax.all_gather(out, "tensor", axis=0, tiled=True)
    tokens_grad = lax.all_gather(xg, "tensor", axis=0, tiled=True)

    def scattered(piece, axis):
        piece = lax.psum_scatter(piece, "tensor", scatter_dimension=0)
        return lax.psum_scatter(piece, "dp", scatter_dimension=axis, tiled=True).astype(F32)

    part0 = scattered(d0, 1)
    part1 = scattered(d1, 0)
    part2 = scattered(d2, 0)
    qv = sums_qv[:, :2].transpose(1, 0, 2).reshape(2, D)
    sums = jnp.concatenate(
        [sums_in[0:1], sums[1:2], sums_in[1:2], qv, sums[5:12]], 0
    )
    sums = lax.psum_scatter(sums, ("dp", "tensor"), scatter_dimension=1, tiled=True)
    return layer_out, tokens_grad, *placed(tie_map, sums, part0, part1, part2)


def fused_step(
    tokens, lengths, tie_map, norm_gains, bias_rows, attention_in, attention_out,
    expand_weight, project_weight, cotangent,
):
    slots = lengths.shape[0]
    tokens = tokens.reshape(slots, -1, D)
    cotangent = cotangent.reshape(slots, -1, D)
    gq, gw, g1, g2, rows, q, v, kt, p, scale, o, a1t, h1, a2, a2t = run_fused_forward(
        tie_map, lengths, tokens, norm_gains, bias_rows, attention_in, attention_out,
        expand_weight, project_weight,
    )
    g1 = g1.reshape(g1.shape[0], D, -1)
    g2 = g2.reshape(g2.shape[0], D, -1)
    out, rest, d1, d2, dh1, gb, gbt, early = run_fused_feed_forward(
        lengths, cotangent, a2, a2t, h1, g1, g2, rows
    )
    grad, rest, part0, partw, part1, part2, sums = run_fused_backward(
        tokens, gq, gw, rows, dh1, gb, gbt, q, v, kt, p, scale, o, a1t, rest, d1, d2, early
    )
    out, grad, *placed_grads = run_place_gradients(
        tie_map, sums, part0, partw, part1, part2, out, rest, grad,
        (norm_gains, bias_rows, attention_in, attention_out, expand_weight, project_weight),
    )
    return out.reshape(-1, D), grad.reshape(-1, D), *placed_grads


def placed(tie_map, sums, part0, part1, part2):
    source = jnp.arange(NSRC, dtype=jnp.int32)

    def place(piece, which):
        pick = (source == tie_map[which]).reshape((NSRC,) + (1,) * piece.ndim)
        return jnp.where(pick, piece[None], 0.0)

    def place_rows(piece, kinds):
        pick = source[:, None] == tie_map[jnp.array(kinds, dtype=jnp.int32)][None, :]
        return jnp.where(pick[:, :, None], piece[None], 0.0)

    return (
        place_rows(sums[:2], [0, 2]),
        place_rows(sums[2:], [0, 0, 0, 1, 2, 3] + [2] * (FF // D)),
        place(part0[:3], 0),
        place(part0[3].T, 1),
        place(part1, 2),
        place(part2.T, 3),
    )


def solution(mesh):
    fused = mesh.shape["dp"] == Z_DEV * Y_DEV and mesh.shape["tensor"] == X_DEV * C_DEV
    return jax.shard_map(
        fused_step if fused else plain_step,
        mesh=mesh,
        in_specs=(
            P("dp", None),
            P("dp"),
            P(),
            P(None, None, ("dp", "tensor")),
            P(None, None, ("dp", "tensor")),
            P(None, None, "dp", "tensor"),
            P(None, "tensor", "dp"),
            P(None, "dp", "tensor"),
            P(None, "tensor", "dp"),
            P("dp", None),
        ),
        out_specs=(
            P("dp", None),
            P("dp", None),
            P(None, None, ("dp", "tensor")),
            P(None, None, ("dp", "tensor")),
            P(None, None, "dp", "tensor"),
            P(None, "tensor", "dp"),
            P(None, "dp", "tensor"),
            P(None, "tensor", "dp"),
        ),
        check_vma=False,
    )
```

```python
import jax
import jax.numpy as jnp
from jax import lax
from jax.experimental import pallas as pl
from jax.experimental.pallas import tpu as pltpu
from jax.sharding import PartitionSpec as P

D = 768
HEAD_DIM = 64
FF = 3072
NSRC = 4
EPS = 1e-05
MASKED = -1e30
F32 = jnp.float32
BF16 = jnp.bfloat16
VMEM_LIMIT = 60 * 1024 * 1024


def dot_nn(a, b):
    return lax.dot_general(a, b, (((1,), (0,)), ((), ())), preferred_element_type=F32)


def dot_nt(a, b):
    return lax.dot_general(a, b, (((1,), (1,)), ((), ())), preferred_element_type=F32)


def norm_parts(v):
    center = jnp.mean(v, -1, keepdims=True)
    centered = v - center
    r = lax.rsqrt(jnp.mean(centered * centered, -1, keepdims=True) + EPS)
    return centered * r, r


def head_mask(shape, h):
    lane = lax.broadcasted_iota(jnp.int32, shape, 1)
    return (lane >= h * HEAD_DIM) & (lane < (h + 1) * HEAD_DIM)


def blocks(total, size):
    return [slice(i * size, (i + 1) * size) for i in range(total // size)]


def attention_forward(
    len_ref, x_ref, g_ref, rows_ref, bqv_ref,
    q_ref, v_ref, kt_ref, p_ref, o_ref, a1t_ref, h1_ref, a2_ref, a2t_ref,
    a1_ref, k_ref, vt_ref, ot_ref, attn_ref,
):
    t = pl.program_id(0)
    n = x_ref.shape[0]
    width = g_ref.shape[-1]
    heads = width // HEAD_DIM
    step = 256
    length = len_ref[0]

    @pl.when(t == 0)
    def _():
        @pl.loop(0, n // step)
        def _(b):
            rows = pl.ds(pl.multiple_of(b * step, step), step)
            xhat, _ = norm_parts(x_ref[rows, :].astype(F32))
            a1 = xhat * rows_ref[0:1, :] + rows_ref[2:3, :]
            a1_ref[rows, :] = a1.astype(BF16)
            a1t_ref[:, rows] = a1.astype(BF16).T
            attn_ref[rows, :] = x_ref[rows, :].astype(F32) + rows_ref[5:6, :]

    @pl.loop(0, n // step)
    def _(b):
        rows = pl.ds(pl.multiple_of(b * step, step), step)
        a1 = a1_ref[rows, :]
        q = (dot_nn(a1, g_ref[0, 0]) + bqv_ref[0, 0:1, :]).astype(BF16)
        q_ref[0, rows, :] = q * jnp.asarray(HEAD_DIM ** -0.5, BF16)
        k = dot_nn(a1, g_ref[0, 1]).astype(BF16)
        k_ref[rows, :] = k
        kt_ref[0, :, rows] = k.T
        v = (dot_nn(a1, g_ref[0, 2]) + bqv_ref[0, 1:2, :]).astype(BF16)
        v_ref[0, rows, :] = v
        vt_ref[:, rows] = v.T

    for h in range(heads):
        k = k_ref[...]
        k = jnp.where(head_mask(k.shape, h), k, jnp.zeros_like(k))
        for b in range(n // step):
            first, last = b * step, (b + 1) * step
            q = q_ref[0, first:last, :]
            key = lax.broadcasted_iota(jnp.int32, (last, step), 0)
            query = lax.broadcasted_iota(jnp.int32, (step, step), 1) + first
            s = dot_nt(k[:last], q)
            near = jnp.where(
                (key[first:] <= query) & (key[first:] < length), s[first:], MASKED
            )
            if b:
                far = jnp.where(key[:first] < length, s[:first], MASKED)
                top = jnp.maximum(
                    jnp.max(far, 0, keepdims=True), jnp.max(near, 0, keepdims=True)
                )
                e_far = jnp.exp(far - top)
                e_near = jnp.exp(near - top)
                total = jnp.sum(e_far, 0, keepdims=True) + jnp.sum(e_near, 0, keepdims=True)
                scale = 1.0 / total
                p_ref[0, h, :first, first:last] = (e_far * scale).astype(BF16)
            else:
                top = jnp.max(near, 0, keepdims=True)
                e_near = jnp.exp(near - top)
                scale = 1.0 / jnp.sum(e_near, 0, keepdims=True)
            p_ref[0, h, first:last, first:last] = (e_near * scale).astype(BF16)
            ot_ref[h * HEAD_DIM : (h + 1) * HEAD_DIM, first:last] = dot_nn(
                vt_ref[h * HEAD_DIM : (h + 1) * HEAD_DIM, :last],
                p_ref[0, h, :last, first:last],
            ).astype(BF16)

    @pl.loop(0, n // step)
    def _(b):
        rows = pl.ds(pl.multiple_of(b * step, step), step)
        o = ot_ref[:, rows].T
        o_ref[0, rows, :] = o
        attn_ref[rows, :] += dot_nt(o, g_ref[0, 3])

    @pl.when(t == pl.num_programs(0) - 1)
    def _():
        @pl.loop(0, n // step)
        def _(b):
            rows = pl.ds(pl.multiple_of(b * step, step), step)
            h1 = attn_ref[rows, :]
            h1_ref[rows, :] = h1
            xhat, _ = norm_parts(h1)
            a2 = (xhat * rows_ref[1:2, :] + rows_ref[6:7, :]).astype(BF16)
            a2_ref[rows, :] = a2
            a2t_ref[:, rows] = a2.T


SQRT_2_PI = 0.7978845608028654


def feed_forward_both(
    len_ref, c_ref, a2_ref, a2t_ref, h1_ref, w1_ref, w2_ref, rows_ref,
    out_ref, d1_ref, d2_ref, dh1_ref, gb_ref, gbt_ref, sums_ref,
    gf_ref, gft_ref, feed_ref, da2_ref, h_ref, df_ref,
):
    t = pl.program_id(0)
    n = c_ref.shape[0]
    step = 256
    length = len_ref[0]

    @pl.when(t == 0)
    def _():
        sums_ref[...] = jnp.zeros_like(sums_ref)

        @pl.loop(0, n // step)
        def _(b):
            rows = pl.ds(pl.multiple_of(b * step, step), step)
            place = b * step + lax.broadcasted_iota(jnp.int32, (step, 1), 0)
            live = (place < length).astype(F32)
            g = (c_ref[rows, :].astype(F32) * live).astype(BF16)
            gf_ref[rows, :] = g
            gft_ref[:, rows] = g.T
            sums_ref[7:8, :] += jnp.sum(g.astype(F32), 0, keepdims=True)

    bias = rows_ref[pl.ds(8 + t, 1), :]

    @pl.loop(0, n // step)
    def _(b):
        rows = pl.ds(pl.multiple_of(b * step, step), step)
        f = dot_nn(a2_ref[rows, :], w1_ref[0]) + bias
        dh = dot_nn(gf_ref[rows, :], w2_ref[0])
        f2 = f * f
        th = jnp.tanh(f * (SQRT_2_PI + (SQRT_2_PI * 0.044715) * f2))
        half = 0.5 + 0.5 * th
        h = (f * half).astype(BF16)
        slope = half + f * (0.5 - 0.5 * th * th) * (
            SQRT_2_PI + (3 * SQRT_2_PI * 0.044715) * f2
        )
        df = (dh * slope).astype(BF16)
        h_ref[rows, :] = h
        df_ref[rows, :] = df
        sums_ref[pl.ds(8 + t, 1), :] += jnp.sum(df.astype(F32), 0, keepdims=True)
        feed = dot_nt(h, w2_ref[0])
        da2 = dot_nt(df, w1_ref[0])

        @pl.when(t == 0)
        def _():
            feed_ref[rows, :] = feed
            da2_ref[rows, :] = da2

        @pl.when(t > 0)
        def _():
            feed_ref[rows, :] += feed
            da2_ref[rows, :] += da2

    @pl.loop(0, D // step)
    def _(b):
        rows = pl.ds(pl.multiple_of(b * step, step), step)
        d1_ref[0, rows, :] = dot_nn(a2t_ref[rows, :], df_ref[...]).astype(BF16)
        d2_ref[0, rows, :] = dot_nn(gft_ref[rows, :], h_ref[...]).astype(BF16)

    @pl.when(t == pl.num_programs(0) - 1)
    def _():
        @pl.loop(0, n // step)
        def _(b):
            rows = pl.ds(pl.multiple_of(b * step, step), step)
            place = b * step + lax.broadcasted_iota(jnp.int32, (step, 1), 0)
            live = (place < length).astype(F32)
            h1 = h1_ref[rows, :]
            out_ref[rows, :] = (live * (h1 + (feed_ref[rows, :] + rows_ref[7:8, :]))).astype(BF16)
            xhat, r = norm_parts(h1)
            da2 = da2_ref[rows, :]
            sums_ref[1:2, :] += jnp.sum(da2 * xhat, 0, keepdims=True)
            sums_ref[6:7, :] += jnp.sum(da2, 0, keepdims=True)
            dg = da2 * rows_ref[1:2, :]
            dv = r * (
                dg
                - jnp.mean(dg, -1, keepdims=True)
                - xhat * jnp.mean(dg * xhat, -1, keepdims=True)
            )
            dh1 = live * c_ref[rows, :].astype(F32) + dv
            dh1_ref[rows, :] = dh1
            gb = dh1.astype(BF16)
            gb_ref[rows, :] = gb
            gbt_ref[:, rows] = gb.T
            sums_ref[5:6, :] += jnp.sum(gb.astype(F32), 0, keepdims=True)


def attention_backward(
    x_ref, g_ref, rows_ref, dh1_ref, gb_ref, gbt_ref, q_ref, v_ref, kt_ref, p_ref,
    o_ref, a1t_ref,
    d0_ref, xg_ref, sums_ref, bqv_ref,
    do_ref, delta_ref, dqt_ref, dq_ref, dk_ref, dv_ref, da1_ref,
):
    t = pl.program_id(0)
    n = x_ref.shape[0]
    width = g_ref.shape[-1]
    heads = width // HEAD_DIM
    step = 256
    pick = (
        lax.broadcasted_iota(jnp.int32, (16, width), 1) // HEAD_DIM
        == lax.broadcasted_iota(jnp.int32, (16, width), 0)
    ).astype(BF16)

    @pl.loop(0, n // step)
    def _(b):
        rows = pl.ds(pl.multiple_of(b * step, step), step)
        do = dot_nn(gb_ref[rows, :], g_ref[0, 3]).astype(BF16)
        do_ref[rows, :] = do
        prod = do.astype(F32) * o_ref[0, rows, :].astype(F32)
        high = prod.astype(BF16)
        low = (prod - high.astype(F32)).astype(BF16)
        delta_ref[:, rows] = dot_nt(pick, high) + dot_nt(pick, low)

    dqt_ref[...] = jnp.zeros_like(dqt_ref)
    for b in range(n // step):
        first, last = b * step, (b + 1) * step
        do = do_ref[first:, :]
        q = q_ref[0, first:, :]
        v = v_ref[0, first:last, :]
        dk, dv = None, None
        for h in range(heads):
            mine = head_mask((1, width), h)
            zero = jnp.zeros((), BF16)
            p = p_ref[0, h, first:last, first:]
            dp = dot_nt(jnp.where(mine, v, zero), do)
            ds = (p.astype(F32) * (dp - delta_ref[h : h + 1, first:])).astype(BF16)
            part = dot_nn(p, jnp.where(mine, do, zero))
            dv = part if dv is None else dv + part
            part = dot_nn(ds, jnp.where(mine, q, zero))
            dk = part if dk is None else dk + part
            head = slice(h * HEAD_DIM, (h + 1) * HEAD_DIM)
            dqt_ref[head, first:] += dot_nn(kt_ref[0, head, first:last], ds)
        dk_ref[first:last, :] = dk.astype(BF16)
        dv_ref[first:last, :] = dv.astype(BF16)

    @pl.when(t == 0)
    def _():
        da1_ref[...] = jnp.zeros_like(da1_ref)

    bqv_ref[...] = jnp.zeros_like(bqv_ref)

    @pl.loop(0, n // step)
    def _(b):
        rows = pl.ds(pl.multiple_of(b * step, step), step)
        dq = (dqt_ref[:, rows] * HEAD_DIM ** -0.5).astype(BF16).T
        dk = dk_ref[rows, :]
        dv = dv_ref[rows, :]
        dq_ref[rows, :] = dq
        bqv_ref[0, 0:1, :] += jnp.sum(dq.astype(F32), 0, keepdims=True)
        bqv_ref[0, 1:2, :] += jnp.sum(dv.astype(F32), 0, keepdims=True)
        da1_ref[rows, :] += (
            dot_nt(dq, g_ref[0, 0]) + dot_nt(dk, g_ref[0, 1]) + dot_nt(dv, g_ref[0, 2])
        )

    @pl.loop(0, D // step)
    def _(b):
        rows = pl.ds(pl.multiple_of(b * step, step), step)
        a1t = a1t_ref[rows, :]
        d0_ref[0, 0, rows, :] = dot_nn(a1t, dq_ref[...]).astype(BF16)
        d0_ref[0, 1, rows, :] = dot_nn(a1t, dk_ref[...]).astype(BF16)
        d0_ref[0, 2, rows, :] = dot_nn(a1t, dv_ref[...]).astype(BF16)
        d0_ref[0, 3, rows, :] = dot_nn(gbt_ref[rows, :], o_ref[0]).astype(BF16)

    @pl.when(t == pl.num_programs(0) - 1)
    def _():
        sums_ref[...] = jnp.zeros_like(sums_ref)

        @pl.loop(0, n // step)
        def _(b):
            rows = pl.ds(pl.multiple_of(b * step, step), step)
            xhat, r = norm_parts(x_ref[rows, :].astype(F32))
            da1 = da1_ref[rows, :]
            sums_ref[0:1, :] += jnp.sum(da1 * xhat, 0, keepdims=True)
            sums_ref[1:2, :] += jnp.sum(da1, 0, keepdims=True)
            dg = da1 * rows_ref[0:1, :]
            dv = r * (
                dg
                - jnp.mean(dg, -1, keepdims=True)
                - xhat * jnp.mean(dg * xhat, -1, keepdims=True)
            )
            xg_ref[rows, :] = (dh1_ref[rows, :] + dv).astype(BF16)


def whole(*shape):
    return pl.BlockSpec(shape, lambda t: (0,) * len(shape))


def group(*shape):
    return pl.BlockSpec((1,) + shape, lambda t: (t,) + (0,) * len(shape))


def shaped(dtype, *shape):
    return jax.ShapeDtypeStruct(shape, dtype)


SMEM_WHOLE = pl.BlockSpec(memory_space=pltpu.SMEM)


def run_attention_forward(length, x, g0, rows, bqv):
    n = x.shape[0]
    groups, _, _, width = g0.shape
    heads = width // HEAD_DIM
    return pl.pallas_call(
        attention_forward,
        grid=(groups,),
        in_specs=[SMEM_WHOLE, whole(n, D), group(4, D, width), whole(16, D), group(2, width)],
        out_specs=[
            group(n, width), group(n, width), group(width, n), group(heads, n, n),
            group(n, width), whole(D, n), whole(n, D), whole(n, D), whole(D, n),
        ],
        out_shape=[
            shaped(BF16, groups, n, width), shaped(BF16, groups, n, width),
            shaped(BF16, groups, width, n), shaped(BF16, groups, heads, n, n),
            shaped(BF16, groups, n, width), shaped(BF16, D, n), shaped(F32, n, D),
            shaped(BF16, n, D), shaped(BF16, D, n),
        ],
        scratch_shapes=[
            pltpu.VMEM((n, D), BF16), pltpu.VMEM((n, width), BF16),
            pltpu.VMEM((width, n), BF16), pltpu.VMEM((width, n), BF16),
            pltpu.VMEM((n, D), F32),
        ],
        compiler_params=pltpu.CompilerParams(vmem_limit_bytes=VMEM_LIMIT),
        name="attention_forward",
    )(length, x, g0, rows, bqv)


def run_feed_forward(length, cot, a2, a2t, h1, g1, g2, rows):
    n = cot.shape[0]
    groups, _, width = g1.shape
    return pl.pallas_call(
        feed_forward_both,
        grid=(groups,),
        in_specs=[
            SMEM_WHOLE, whole(n, D), whole(n, D), whole(D, n), whole(n, D),
            group(D, width), group(D, width), whole(16, D),
        ],
        out_specs=[
            whole(n, D), group(D, width), group(D, width), whole(n, D), whole(n, D),
            whole(D, n), whole(16, D),
        ],
        out_shape=[
            shaped(BF16, n, D), shaped(BF16, groups, D, width), shaped(BF16, groups, D, width),
            shaped(F32, n, D), shaped(BF16, n, D), shaped(BF16, D, n), shaped(F32, 16, D),
        ],
        scratch_shapes=[
            pltpu.VMEM((n, D), BF16), pltpu.VMEM((D, n), BF16), pltpu.VMEM((n, D), F32),
            pltpu.VMEM((n, D), F32), pltpu.VMEM((n, width), BF16), pltpu.VMEM((n, width), BF16),
        ],
        compiler_params=pltpu.CompilerParams(vmem_limit_bytes=VMEM_LIMIT),
        name="feed_forward_both",
    )(length, cot, a2, a2t, h1, g1, g2, rows)


def run_attention_backward(x, g0, rows, dh1, gb, gbt, q, v, kt, p, o, a1t):
    n = x.shape[0]
    groups, _, _, width = g0.shape
    heads = width // HEAD_DIM
    return pl.pallas_call(
        attention_backward,
        grid=(groups,),
        in_specs=[
            whole(n, D), group(4, D, width), whole(16, D), whole(n, D), whole(n, D),
            whole(D, n), group(n, width), group(n, width), group(width, n),
            group(heads, n, n), group(n, width), whole(D, n),
        ],
        out_specs=[group(4, D, width), whole(n, D), whole(8, D), group(8, width)],
        out_shape=[
            shaped(BF16, groups, 4, D, width), shaped(BF16, n, D), shaped(F32, 8, D),
            shaped(F32, groups, 8, width),
        ],
        scratch_shapes=[
            pltpu.VMEM((n, width), BF16), pltpu.VMEM((16, n), F32), pltpu.VMEM((width, n), F32),
            pltpu.VMEM((n, width), BF16), pltpu.VMEM((n, width), BF16),
            pltpu.VMEM((n, width), BF16), pltpu.VMEM((n, D), F32),
        ],
        compiler_params=pltpu.CompilerParams(vmem_limit_bytes=VMEM_LIMIT),
        name="attention_backward",
    )(x, g0, rows, dh1, gb, gbt, q, v, kt, p, o, a1t)


Z_DEV, Y_DEV, X_DEV, C_DEV = 4, 2, 2, 2


class Place:
    def __init__(self):
        dp, self.t = lax.axis_index("dp"), lax.axis_index("tensor")
        self.dp = dp
        self.z, self.y = dp // 2, dp % 2
        self.x, self.c = self.t // 2, self.t % 2
        self.other_y = 1 - self.y
        self.zs = [
            self.z,
            self.z + 1 - 2 * (self.z % 2),
            self.z + 2 - 4 * (self.z // 2),
            3 - self.z,
        ]
        self.ts = [
            self.t,
            self.t + 1 - 2 * (self.t % 2),
            self.t + 2 - 4 * (self.t // 2),
            3 - self.t,
        ]
        self.to_z = [dict(dp=z * 2 + self.y) for z in self.zs]
        self.to_y = dict(dp=self.z * 2 + self.other_y)
        self.to_x = dict(tensor=self.ts[2])
        self.to_core = dict(tensor=self.ts[1])

    def group(self, k):
        return lax.select(
            k == 0, self.ts[0],
            lax.select(k == 1, self.ts[1], lax.select(k == 2, self.ts[2], self.ts[3])),
        )

    def greet(self):
        barrier = pltpu.get_barrier_semaphore()
        others = self.to_z[1:] + [self.to_y, self.to_x, self.to_core]
        for device in others:
            pl.semaphore_signal(
                barrier, inc=1, device_id=device, device_id_type=pl.DeviceIdType.MESH
            )
        pl.semaphore_wait(barrier, len(others))


class Links:
    def __init__(self, send_sem, recv_sem):
        self.send_sem, self.recv_sem = send_sem, recv_sem
        self.copies = []

    def add(self, device, src, dst):
        number = len(self.copies)
        copy = pltpu.make_async_remote_copy(
            src_ref=src,
            dst_ref=dst,
            send_sem=self.send_sem.at[number],
            recv_sem=self.recv_sem.at[number],
            device_id=device,
            device_id_type=pl.DeviceIdType.MESH,
        )
        self.copies.append(copy)
        return copy

    def sent(self, *apart):
        for copy in self.copies:
            if all(copy is not other for other in apart):
                copy.wait_send()


def flat(copies):
    for item in copies:
        if isinstance(item, list):
            yield from flat(item)
        else:
            yield item


def start(*copies):
    for copy in flat(copies):
        copy.start()


def recv(*copies):
    for copy in flat(copies):
        copy.wait_recv()


class Gather:
    def __init__(self, links, place, own, full, x_first, single=True, last=True):
        every = slice(None)
        y, other = place.y, place.other_y

        def same(device, k, yy, to):
            return links.add(device, full(k, every, yy), full(to, every, yy))

        if x_first:
            self.first = [links.add(place.to_x, own, full(2, place.z, y))]
        self.z = [
            links.add(place.to_z[k], own, full(0, place.z, y)) for k in range(1, 4)
        ]
        if x_first:
            far = full(2, place.z, y)
            self.far = [links.add(place.to_z[k], far, far) for k in range(1, 4)]
            self.second = [same(place.to_y, 0, y, 0)]
            if last:
                self.second.append(same(place.to_y, 2, y, 2))
            blocks = [(0, y), (2, y), (0, other), (2, other)]
        else:
            if single:
                self.first = [same(place.to_y, 0, y, 0)]
            else:
                self.first = [links.add(place.to_y, own, full(0, place.z, y))]
                for k in range(1, 4):
                    block = full(0, place.zs[k], y)
                    self.first.append(links.add(place.to_y, block, block))
            self.second = [same(place.to_x, 0, y, 2)]
            if last:
                self.second.append(same(place.to_x, 0, other, 2))
            blocks = [(0, y), (0, other), (2, y), (2, other)]
        blocks = blocks if last else blocks[:-1]
        self.core = [same(place.to_core, k, yy, k + 1) for k, yy in blocks]


def fused_forward(
    tie_ref, len_ref, tokens_ref, gains_ref, bias_ref, in_ref, out_ref, expand_ref,
    project_ref,
    gq_ref, gw_ref, flat1_ref, flat2_ref, rows_ref,
    q_ref, v_ref, kt_ref, p_ref, scale_ref, o_ref, a1t_ref, h1_ref, a2_ref, a2t_ref,
    own0_ref, ownw_ref, own1_ref, own2_ref, square_ref, vec_ref,
    all0_ref, allw_ref, w1_ref, w2_ref, vecs_ref, bqv_ref, x_ref, a1_ref, k_ref, qa_ref, vt_ref,
    ot_ref,
    send_sem, recv_sem, local_sem,
):
    t = pl.program_id(0)
    n, _ = x_ref.shape
    width = allw_ref.shape[-1]
    heads = width // HEAD_DIM
    step = 256
    place = Place()
    length = len_ref[place.t]
    links = Links(send_sem, recv_sem)
    z, y, x, c = place.z, place.y, place.x, place.c
    vec_z = [
        links.add(place.to_z[k], vec_ref, vecs_ref.at[z, y, x, c]) for k in range(1, 4)
    ]
    vec_y = links.add(place.to_y, vecs_ref.at[:, y, x, c], vecs_ref.at[:, y, x, c])
    vec_x = links.add(place.to_x, vecs_ref.at[:, :, x, c], vecs_ref.at[:, :, x, c])
    vec_core = links.add(place.to_core, vecs_ref.at[:, :, :, c], vecs_ref.at[:, :, :, c])
    seg0 = Gather(
        links, place, own0_ref, lambda k, z, y: all0_ref.at[k, z, y], False, False
    )
    segw = Gather(links, place, ownw_ref, lambda k, z, y: allw_ref.at[k, z, y], False)
    seg1 = Gather(
        links, place, own1_ref, lambda k, z, y: w1_ref.at[k, z, y], False, last=False
    )
    seg2 = Gather(
        links, place, own2_ref, lambda k, z, y: w2_ref.at[k, z, y], True, last=False
    )
    flush = [
        pltpu.make_async_copy(w1_ref, flat1_ref, local_sem.at[0]),
        pltpu.make_async_copy(w2_ref, flat2_ref, local_sem.at[1]),
    ]
    fetch = pltpu.make_async_copy(tokens_ref.at[place.t], x_ref, local_sem.at[2])

    def pass_on(seg, stage):
        if stage == 0:
            recv(seg.z)
            start(seg.first, seg.second[0], seg.core[0])
        elif stage == 1:
            recv(seg.first)
            start(seg.second[1:], seg.core[1])
        else:
            recv(seg.second[stage - 2])
            start(seg.core[stage])

    @pl.when(t == 0)
    def _():
        s0, s1, s2, s3 = tie_ref[0], tie_ref[1], tie_ref[2], tie_ref[3]
        fetch.start()
        square_ref[...] = jnp.zeros_like(square_ref)
        gain = gains_ref.shape[-1]
        square_ref[0:1, :gain] = gains_ref[s0].astype(F32)[0:1]
        square_ref[1:2, :gain] = gains_ref[s2].astype(F32)[1:2]
        kinds = [s0, s0, s0, s1, s2, s3, s2, s2, s2, s2]
        for i, source in enumerate(kinds):
            wide = bias_ref[i].astype(F32)
            here = lax.broadcasted_iota(jnp.int32, wide.shape, 0) == source
            square_ref[2 + i : 3 + i, :gain] = jnp.sum(
                jnp.where(here, wide, 0.0), 0, keepdims=True
            )
        vec_ref[...] = square_ref[...].T[:gain]
        for j in range(3):
            own0_ref[:, j * width : (j + 1) * width] = in_ref[s0, j]
        place.greet()
        start(vec_z, seg0.z[1], seg0.z[2], seg0.z[0], seg0.first[0])
        vecs_ref[z, y, x, c] = vec_ref[...]
        all0_ref[0, z, y] = own0_ref[...]
        ownw_ref[...] = out_ref[s1].T
        allw_ref[0, z, y] = ownw_ref[...]
        own1_ref[...] = expand_ref[s2]
        own2_ref[...] = project_ref[s3]
        w1_ref[0, z, y] = own1_ref[...]
        w2_ref[0, z, y] = own2_ref[...]
        recv(vec_z)
        start(vec_y)
        recv(seg0.z[0])
        start(seg0.first[1])
        recv(vec_y)
        start(vec_x)
        recv(vec_x)
        start(vec_core)
        recv(seg0.z[1])
        start(seg0.first[2])
        start(segw.z, seg2.first, seg1.z, seg2.z)
        recv(vec_core)
        vecs = vecs_ref[...].reshape(D, vecs_ref.shape[-1]).T[:16]
        rows_ref[...] = vecs
        for k in range(4):
            part = slice(k * width, (k + 1) * width)
            bqv_ref[k, 0:1, :width] = vecs[3:4, part]
            bqv_ref[k, 0:1, width : 2 * width] = jnp.zeros((1, width), F32)
            bqv_ref[k, 0:1, 2 * width :] = vecs[4:5, part]
        fetch.wait()

        @pl.loop(0, n // step)
        def _(b):
            rows = pl.ds(pl.multiple_of(b * step, step), step)
            wide = x_ref[rows, :].astype(F32)
            xhat, _ = norm_parts(wide)
            a1 = (xhat * rows_ref[0:1, :] + rows_ref[2:3, :]).astype(BF16)
            a1_ref[rows, :] = a1
            a1t_ref[:, rows] = a1.T
            h1_ref[rows, :] = wide + rows_ref[5:6, :]

        recv(seg0.z[2])
        start(seg0.first[3], seg0.second[0], seg0.core[0])
        recv(seg0.first)
        start(seg0.second[1], seg0.core[1])
        pass_on(segw, 0)

    @pl.when(t == 1)
    def _():
        recv(seg0.core[0], seg0.core[1])

    @pl.when(t == 2)
    def _():
        recv(seg2.z)
        start(seg2.second[0], seg2.core[0])
        pass_on(segw, 3)

    @pl.when(t == 3)
    def _():
        recv(seg0.core[2], seg0.core[3])
        pass_on(seg1, 2)
        recv(seg2.far)
        start(seg2.core[1])
        pass_on(seg2, 2)

    gq_ref[0] = all0_ref[t].reshape(gq_ref.shape[1:])
    mine = place.group(t)
    qkv = dot_nn(a1_ref[...], gq_ref[0]) + bqv_ref[mine, 0:1, :]
    q = qkv[:, :width].astype(BF16)
    k = qkv[:, width : 2 * width].astype(BF16)
    v = qkv[:, 2 * width :].astype(BF16)
    q = q * jnp.asarray(HEAD_DIM ** -0.5, BF16)
    q_ref[0] = q
    kt_ref[0] = k.T
    v_ref[0] = v
    vt_ref[...] = v.T
    spare = k_ref.shape[1] - width
    extra = lax.broadcasted_iota(jnp.int32, (n, spare), 1) == 0
    dead = lax.broadcasted_iota(jnp.int32, (n, spare), 0) >= length
    k_ref[:, :width] = k
    k_ref[:, width:] = jnp.where(extra & dead, MASKED, 0.0).astype(BF16)
    qa_ref[:, :width] = q
    qa_ref[:, width:] = jnp.where(extra, 1.0, 0.0).astype(BF16)

    units = [(h, b) for h in range(heads) for b in range(n // step)]

    def scores(h, b):
        first, last = b * step, (b + 1) * step
        q = qa_ref[first:last, :]
        lane = lax.broadcasted_iota(jnp.int32, (1, q.shape[1]), 1)
        keep = head_mask((1, q.shape[1]), h) | (lane >= width)
        return dot_nt(k_ref[:last, :], jnp.where(keep, q, jnp.zeros((), BF16)))

    def attend(h, b, s):
        first, last = b * step, (b + 1) * step
        key = lax.broadcasted_iota(jnp.int32, (step, step), 0)
        query = lax.broadcasted_iota(jnp.int32, (step, step), 1)
        near = jnp.where(key <= query, s[first:], MASKED)
        head = slice(h * HEAD_DIM, (h + 1) * HEAD_DIM)
        top = jnp.max(near, 0, keepdims=True)
        if b:
            far = s[:first]
            top = jnp.maximum(top, jnp.max(far, 0, keepdims=True))
        e_near = jnp.exp(near - top)
        total = jnp.sum(e_near, 0, keepdims=True)
        e_near = e_near.astype(BF16)
        p_ref[0, h, first:last, first:last] = e_near
        o = dot_nn(vt_ref[head, first:last], e_near)
        if b:
            e_far = jnp.exp(far - top)
            total += jnp.sum(e_far, 0, keepdims=True)
            e_far = e_far.astype(BF16)
            p_ref[0, h, :first, first:last] = e_far
            o += dot_nn(vt_ref[head, :first], e_far)
        scale = 1.0 / total
        scale_ref[0, h : h + 1, first:last] = scale
        ot_ref[head, first:last] = (o * scale).astype(BF16)

    scale_ref[0, heads:, :] = jnp.zeros((scale_ref.shape[1] - heads, n), F32)
    s = scores(*units[0])
    for i, unit in enumerate(units):
        ahead = scores(*units[i + 1]) if i + 1 < len(units) else None
        attend(*unit, s)
        s = ahead

    @pl.when(t == 0)
    def _():
        pass_on(seg0, 2)
        pass_on(segw, 1)
        pass_on(seg1, 0)

    @pl.when(t == 1)
    def _():
        pass_on(seg0, 3)
        recv(seg2.first)
        start(seg2.far)
        pass_on(seg1, 1)
        recv(segw.core[0], segw.core[1])

    @pl.when(t == 2)
    def _():
        pass_on(segw, 2)

    @pl.when(t == 3)
    def _():
        recv(segw.core[2], segw.core[3])

    gw_ref[0] = allw_ref[t].reshape(gw_ref.shape[1:])
    o = ot_ref[...].T
    o_ref[0] = o
    h1_ref[...] += dot_nt(o, gw_ref[0])

    @pl.when(t == 3)
    def _():
        @pl.loop(0, n // step)
        def _(b):
            rows = pl.ds(pl.multiple_of(b * step, step), step)
            h1 = h1_ref[rows, :]
            xhat, _ = norm_parts(h1)
            a2 = (xhat * rows_ref[1:2, :] + rows_ref[6:7, :]).astype(BF16)
            a2_ref[rows, :] = a2
            a2t_ref[:, rows] = a2.T

        recv(seg1.core)
        flush[0].start()
        recv(seg2.core)
        flush[1].start()
        links.sent()
        for copy in flush:
            copy.wait()


N_GATHER = 6 + 13 + 10 + 8 + 11
VMEM_WHOLE = pl.BlockSpec(memory_space=pltpu.VMEM)
ANY_WHOLE = pl.BlockSpec(memory_space=pl.ANY)


def run_fused_forward(tie, lengths, tokens, gains, biases, w_in, w_out, w_expand, w_project):
    groups, n, _ = tokens.shape
    depth, width = w_in.shape[-2:]
    heads = width // HEAD_DIM
    hidden = w_expand.shape[-1]
    w_project = w_project.transpose(0, 2, 1)
    biases = biases.transpose(1, 0, 2)
    own = gains.shape[-1]
    return pl.pallas_call(
        fused_forward,
        grid=(groups,),
        in_specs=[SMEM_WHOLE, SMEM_WHOLE, ANY_WHOLE] + [VMEM_WHOLE] * 6,
        out_specs=[
            group(D, 3 * width), group(D, width), ANY_WHOLE, ANY_WHOLE, VMEM_WHOLE,
            group(n, width), group(n, width), group(width, n), group(heads, n, n),
            group(8, n), group(n, width), VMEM_WHOLE, VMEM_WHOLE, VMEM_WHOLE, VMEM_WHOLE,
        ],
        out_shape=[
            shaped(BF16, groups, D, 3 * width), shaped(BF16, groups, D, width),
            shaped(BF16, groups, Z_DEV, Y_DEV, depth, hidden),
            shaped(BF16, groups, Z_DEV, Y_DEV, depth, hidden),
            shaped(F32, 16, D),
            shaped(BF16, groups, n, width), shaped(BF16, groups, n, width),
            shaped(BF16, groups, width, n), shaped(BF16, groups, heads, n, n),
            shaped(F32, groups, 8, n), shaped(BF16, groups, n, width), shaped(BF16, D, n), shaped(F32, n, D),
            shaped(BF16, n, D), shaped(BF16, D, n),
        ],
        scratch_shapes=[
            pltpu.VMEM((depth, 3 * width), BF16), pltpu.VMEM((depth, width), BF16),
            pltpu.VMEM((depth, hidden), BF16), pltpu.VMEM((depth, hidden), BF16),
            pltpu.VMEM((128, 128), F32), pltpu.VMEM((own, 128), F32),
            pltpu.VMEM((groups, Z_DEV, Y_DEV, depth, 3 * width), BF16),
            pltpu.VMEM((groups, Z_DEV, Y_DEV, depth, width), BF16),
            pltpu.VMEM((groups, Z_DEV, Y_DEV, depth, hidden), BF16),
            pltpu.VMEM((groups, Z_DEV, Y_DEV, depth, hidden), BF16),
            pltpu.VMEM((Z_DEV, Y_DEV, X_DEV, C_DEV, own, 128), F32),
            pltpu.VMEM((groups, 8, 3 * width), F32),
            pltpu.VMEM((n, D), BF16), pltpu.VMEM((n, D), BF16), pltpu.VMEM((n, 256), BF16),
            pltpu.VMEM((n, 256), BF16), pltpu.VMEM((width, n), BF16),
            pltpu.VMEM((width, n), BF16),
            pltpu.SemaphoreType.DMA((N_GATHER,)), pltpu.SemaphoreType.DMA((N_GATHER,)),
            pltpu.SemaphoreType.DMA((3,)),
        ],
        compiler_params=pltpu.CompilerParams(
            vmem_limit_bytes=VMEM_LIMIT, collective_id=0, has_side_effects=True
        ),
        name="fused_forward",
    )(tie, lengths, tokens, gains, biases, w_in, w_out, w_expand, w_project)


class Result:
    def __init__(self, links, place, own_ref, passing_ref, out_ref, step, sem):
        count = own_ref.shape[0] // step
        self.own_ref, self.passing_ref, self.out_ref, self.sem = own_ref, passing_ref, out_ref, sem
        self.place = place
        self.x, self.core, self.far = [], [], []
        for i in range(count):
            rows = pl.ds(i * step, step)
            mine, theirs = out_ref.at[place.t, rows], out_ref.at[place.ts[2], rows]
            self.x.append(links.add(place.to_x, own_ref.at[rows], passing_ref.at[rows]))
            self.core.append(links.add(place.to_core, own_ref.at[rows], mine))
            self.far.append(links.add(place.to_core, passing_ref.at[rows], theirs))

    def send(self, i):
        start(self.x[i], self.core[i])

    def pass_on(self, i):
        recv(self.x[i])
        start(self.far[i])

    def finish(self):
        for ref, where in [
            (self.own_ref, self.place.t), (self.passing_ref, self.place.ts[2])
        ]:
            copy = pltpu.make_async_copy(ref, self.out_ref.at[where], self.sem)
            copy.start()
            copy.wait()
        recv(self.core, self.far)


def pair_order(i):
    return i + 1 - 2 * (i % 2)


def fused_feed_forward(
    len_ref, cot_ref, a2_ref, a2t_ref, h1_ref, far1_ref, far2_ref, w1_ref, w2_ref, rows_ref,
    out_ref, fold_ref, work_ref, dh1_ref, gb_ref, gbt_ref, sums_ref,
    gf_ref, gft_ref, feed_ref, da2_ref, h_ref, df_ref, whole_ref, missing_ref,
    stage_ref, land_ref, near_ref, cross_ref,
    send_sem, recv_sem, local_sem,
):
    t = pl.program_id(0)
    n = gf_ref.shape[0]
    step = 256
    depth = stage_ref.shape[-2]
    place = Place()
    length = len_ref[place.t]
    links = Links(send_sem, recv_sem)
    y, other = place.y, place.other_y
    last = [
        links.add(place.to_x, far1_ref.at[0, :, other], missing_ref.at[0, 0]),
        links.add(place.to_y, far2_ref.at[2, :, y], missing_ref.at[1, 0]),
    ]
    last_core = [
        links.add(place.to_core, missing_ref.at[i, 0], missing_ref.at[i, 1]) for i in range(2)
    ]
    core = [
        [links.add(place.to_core, stage_ref.at[i], land_ref.at[s, i]) for i in range(2)]
        for s in range(2)
    ]
    cross = [
        links.add(place.to_y, near_ref.at[i, :, other], cross_ref.at[i]) for i in range(2)
    ]
    fetch = pltpu.make_async_copy(cot_ref.at[place.t], gf_ref, local_sem)
    k = pair_order(t)
    mine = place.group(k)

    def live_rows(b):
        at = b * step + lax.broadcasted_iota(jnp.int32, (step, 1), 0)
        return (at < length).astype(F32)

    @pl.when(t == 0)
    def _():
        fetch.start()
        place.greet()
        start(last)
        sums_ref[...] = jnp.zeros_like(sums_ref)
        feed_ref[...] = jnp.zeros_like(feed_ref)
        da2_ref[...] = jnp.zeros_like(da2_ref)
        fetch.wait()

        @pl.loop(0, n // step)
        def _(b):
            rows = pl.ds(pl.multiple_of(b * step, step), step)
            g = (gf_ref[rows, :].astype(F32) * live_rows(b)).astype(BF16)
            gf_ref[rows, :] = g
            gft_ref[:, rows] = g.T
            sums_ref[7:8, :] += jnp.sum(g.astype(F32), 0, keepdims=True)

    @pl.when(t < 2)
    def _():
        whole_ref[0] = w1_ref[0]
        whole_ref[1] = w2_ref[0]

    @pl.when(t == 2)
    def _():
        recv(last_core)

    @pl.when(t >= 2)
    def _():
        whole_ref[0, :, y] = w1_ref[0, :, y]
        whole_ref[1, :, y] = w2_ref[0, :, y]
        for i in range(2):
            whole_ref[i, :, other] = missing_ref[i, 3 - t]

    bias = rows_ref[pl.ds(8 + mine, 1), :]
    w1 = whole_ref[0].reshape(D, -1)
    w2 = whole_ref[1].reshape(D, -1)
    column = jnp.zeros((1, w1.shape[1]), F32)
    for rows in blocks(n, step):
        f = dot_nn(a2_ref[rows, :], w1) + bias
        dh = dot_nn(gf_ref[rows, :], w2)
        f2 = f * f
        th = jnp.tanh(f * (SQRT_2_PI + (SQRT_2_PI * 0.044715) * f2))
        half = 0.5 + 0.5 * th
        h = (f * half).astype(BF16)
        slope = half + f * (0.5 - 0.5 * th * th) * (
            SQRT_2_PI + (3 * SQRT_2_PI * 0.044715) * f2
        )
        df = (dh * slope).astype(BF16)
        h_ref[rows, :] = h
        df_ref[rows, :] = df
        column += jnp.sum(df.astype(F32), 0, keepdims=True)
        feed_ref[rows, :] += dot_nt(h, w2)
        da2_ref[rows, :] += dot_nt(df, w1)
    sums_ref[pl.ds(8 + mine, 1), :] = column

    @pl.when(t == 1)
    def _():
        recv(last)
        start(last_core)

    def weight_grad(left_ref, right_ref):
        value = dot_nn(left_ref[...], right_ref[...])
        return value.reshape(Z_DEV, Y_DEV, depth, value.shape[-1]).astype(BF16)

    grad1 = weight_grad(a2t_ref, df_ref)
    grad2 = weight_grad(gft_ref, h_ref)

    def put(ref):
        ref[0] = grad1
        ref[1] = grad2

    def reduced(ref):
        return lambda i, s, z: (
            ref[i, z].astype(F32) + land_ref[s, i, z].astype(F32)
        ).astype(BF16)

    @pl.when(t == 0)
    def _():
        put(stage_ref)
        start(core[0])

    @pl.when(t == 1)
    def _():
        put(near_ref)

    @pl.when(t == 2)
    def _():
        for copy in core[0]:
            copy.wait_send()
        put(stage_ref)
        start(core[1])
        recv(core[0])

        @pl.loop(0, Z_DEV)
        def _(z):
            for i in range(2):
                near_ref[i, z] = reduced(near_ref)(i, 0, z)

        start(cross)

    @pl.when(t == 3)
    def _():
        put(work_ref)

        @pl.loop(0, n // step)
        def _(b):
            rows = pl.ds(pl.multiple_of(b * step, step), step)
            live = live_rows(b)
            h1 = h1_ref[rows, :]
            out_ref[rows, :] = (live * (h1 + (feed_ref[rows, :] + rows_ref[7:8, :]))).astype(BF16)
            xhat, r = norm_parts(h1)
            da2 = da2_ref[rows, :]
            sums_ref[1:2, :] += jnp.sum(da2 * xhat, 0, keepdims=True)
            sums_ref[6:7, :] += jnp.sum(da2, 0, keepdims=True)
            dg = da2 * rows_ref[1:2, :]
            dv = r * (
                dg
                - jnp.mean(dg, -1, keepdims=True)
                - xhat * jnp.mean(dg * xhat, -1, keepdims=True)
            )
            dh1 = gf_ref[rows, :].astype(F32) + dv
            dh1_ref[rows, :] = dh1
            gb = dh1.astype(BF16)
            gb_ref[rows, :] = gb
            gbt_ref[:, rows] = gb.T
            sums_ref[5:6, :] += jnp.sum(gb.astype(F32), 0, keepdims=True)

        recv(core[1])

        @pl.loop(0, Z_DEV)
        def _(z):
            for i in range(2):
                work_ref[i, z] = reduced(work_ref)(i, 1, z)

        recv(cross)

        @pl.loop(0, Z_DEV)
        def _(z):
            for i in range(2):
                fold_ref[i, z] = (
                    near_ref[i, z, y].astype(F32) + cross_ref[i, z].astype(F32)
                ).astype(BF16)

        links.sent(*core[0])


def run_fused_feed_forward(lengths, cot, a2, a2t, h1, g1, g2, rows):
    n = cot.shape[1]
    groups, _, _, depth, hidden = g1.shape
    both = (2, Z_DEV, Y_DEV, depth, hidden)
    fold = (2, Z_DEV, depth, hidden)
    weight = pl.BlockSpec(
        (1, Z_DEV, Y_DEV, depth, hidden), lambda t: (pair_order(t), 0, 0, 0, 0)
    )
    return pl.pallas_call(
        fused_feed_forward,
        grid=(groups,),
        in_specs=[SMEM_WHOLE, ANY_WHOLE] + [VMEM_WHOLE] * 3 + [ANY_WHOLE] * 2
        + [weight, weight, VMEM_WHOLE],
        out_specs=[VMEM_WHOLE] * 7,
        out_shape=[
            shaped(BF16, n, D), shaped(BF16, *fold), shaped(BF16, *both), shaped(F32, n, D),
            shaped(BF16, n, D), shaped(BF16, D, n), shaped(F32, 16, D),
        ],
        scratch_shapes=[
            pltpu.VMEM((n, D), BF16), pltpu.VMEM((D, n), BF16), pltpu.VMEM((n, D), F32),
            pltpu.VMEM((n, D), F32), pltpu.VMEM((n, hidden), BF16), pltpu.VMEM((n, hidden), BF16),
            pltpu.VMEM(both, BF16), pltpu.VMEM((2,) + fold, BF16),
            pltpu.VMEM(both, BF16), pltpu.VMEM((2,) + both, BF16),
            pltpu.VMEM(both, BF16), pltpu.VMEM(fold, BF16),
            pltpu.SemaphoreType.DMA((10,)), pltpu.SemaphoreType.DMA((10,)),
            pltpu.SemaphoreType.DMA,
        ],
        compiler_params=pltpu.CompilerParams(
            vmem_limit_bytes=VMEM_LIMIT, collective_id=1, has_side_effects=True
        ),
        name="fused_feed_forward",
    )(lengths, cot, a2, a2t, h1, g1, g2, g1, g2, rows)
class Reduce:
    def __init__(
        self, links, place, work, acc, cross_ref, far_ref, last_ref, side_ref, slots=(0, 1)
    ):
        self.place, self.work, self.acc = place, work, acc
        self.cross_ref, self.far_ref = cross_ref, far_ref
        self.last_ref, self.side_ref = last_ref, side_ref
        zs = place.zs
        self.y = {
            s: [
                links.add(place.to_y, work(s, zs[j], place.other_y), cross_ref.at[s, zs[j]])
                for j in (1, 2, 3, 0)
            ]
            for s in slots
        }
        self.z = [
            [
                links.add(place.to_z[j], acc(s, zs[j]), far_ref.at[s, j - 1])
                for j in range(1, 4)
            ]
            for s in range(2)
        ]
        self.x = links.add(place.to_x, last_ref, side_ref)

    def fold_y(self, s):
        for i, j in enumerate((1, 2, 3, 0)):
            z = self.place.zs[j]
            recv(self.y[s][i])
            value = self.work(s, z, self.place.y)[...].astype(F32)
            self.acc(s, z)[...] = (value + self.cross_ref[s, z].astype(F32)).astype(BF16)
            if j:
                start(self.z[s][j - 1])

    def own(self, s):
        recv(self.z[s])
        far = self.far_ref
        return self.acc(s, self.place.z)[...].astype(F32) + (
            far[s, 0].astype(F32) + far[s, 1].astype(F32) + far[s, 2].astype(F32)
        )

    def send_x(self):
        self.last_ref[...] = self.own(1).astype(BF16)
        start(self.x)

    def total(self):
        value = self.own(0)
        recv(self.x)
        return value + self.side_ref[...].astype(F32)


def fused_backward(
    tokens_ref, gq_ref, gw_ref, rows_ref, dh1_ref, gb_ref, gbt_ref, q_ref, v_ref, kt_ref,
    p_ref, scale_ref, o_ref, a1t_ref, layer_ref, fold_ref, work_ref, early_ref,
    out_ref, layerout_ref, part0_ref, partw_ref, part1_ref, part2_ref, total_ref,
    do_ref, delta_ref, dqt_ref, dqkv_ref, da1_ref, own_ref, passing_ref, passlayer_ref, bqv_ref,
    folded_ref, cross1_ref, far1_ref, last1_ref, side1_ref,
    cross2_ref, far2_ref, last2_ref, side2_ref,
    stagew_ref, landw_ref, workw_ref, crossw_ref, farw_ref, lastw_ref, sidew_ref,
    stage0_ref, land0_ref, work0_ref, cross0_ref, far0_ref, last0_ref, side0_ref,
    sums_ref, sumland_ref,
    send_sem, recv_sem, local_sem,
):
    t = pl.program_id(0)
    n = own_ref.shape[0]
    width = gw_ref.shape[-1]
    depth = part0_ref.shape[0]
    heads = width // HEAD_DIM
    step = n // 4
    place = Place()
    y = place.y
    links = Links(send_sem, recv_sem)
    k, b = group_and_block(t)
    mine = place.group(k)
    out = Result(links, place, own_ref, passing_ref, out_ref, step, local_sem.at[0])
    layer = Result(links, place, layer_ref, passlayer_ref, layerout_ref, step, local_sem.at[1])
    fetch = pltpu.make_async_copy(tokens_ref.at[place.t], own_ref, local_sem.at[2])
    corew = [links.add(place.to_core, stagew_ref.at[i], landw_ref.at[i]) for i in range(2)]
    core0 = [links.add(place.to_core, stage0_ref.at[i], land0_ref.at[i]) for i in range(2)]
    def half_done(i, *landing):
        return Reduce(
            links, place, lambda s, z, y: work_ref.at[i, z, y],
            lambda s, z: folded_ref.at[i, z] if s else fold_ref.at[i, z],
            *landing, slots=(1,),
        )

    seg1 = half_done(0, cross1_ref, far1_ref, last1_ref, side1_ref)
    seg2 = half_done(1, cross2_ref, far2_ref, last2_ref, side2_ref)
    segw = Reduce(
        links, place, lambda s, z, y: workw_ref.at[s, z, y],
        lambda s, z: workw_ref.at[s, z, y],
        crossw_ref, farw_ref, lastw_ref, sidew_ref,
    )
    seg0 = Reduce(
        links, place, lambda s, z, y: work0_ref.at[s, z, y],
        lambda s, z: work0_ref.at[s, z, y],
        cross0_ref, far0_ref, last0_ref, side0_ref,
    )
    sum_core, sum_y, *sum_z, sum_x = [
        links.add(to, sums_ref.at[i], sumland_ref.at[j])
        for j, (i, to) in enumerate(
            zip([0, 1, 2, 2, 2, 3], [place.to_core, place.to_y] + place.to_z[1:] + [place.to_x])
        )
    ]

    def when(now):
        return pl.when(t == now)

    @when(0)
    def _():
        fetch.start()
        place.greet()
        for i in range(4):
            layer.send(i)
        start(seg1.y[1], seg2.y[1], seg1.z[0], seg2.z[0])
        bqv_ref[...] = jnp.zeros_like(bqv_ref)
        sums_ref[0] = early_ref[...]
        da1_ref[...] = jnp.zeros_like(da1_ref)
        fetch.wait()

    for i, now in enumerate([4, 6, 9, 11]):
        @when(now)
        def _():
            layer.pass_on(i)

    @when(5)
    def _():
        seg1.fold_y(1)

    @when(9)
    def _():
        seg2.fold_y(1)

    @when(10)
    def _():
        segw.fold_y(0)

    @when(11)
    def _():
        recv(corew[1])

        @pl.loop(0, Z_DEV)
        def _(z):
            workw_ref[1, z] = (
                workw_ref[1, z].astype(F32) + landw_ref[1, z].astype(F32)
            ).astype(BF16)

        start(segw.y[1])

    @when(13)
    def _():
        seg0.fold_y(0)
        seg1.send_x()

    @when(15)
    def _():
        segw.fold_y(1)
        out.pass_on(0)

    @pl.when((t == 0) | (t == 4) | (t == 8) | (t == 9))
    def _():
        pick = (
            lax.broadcasted_iota(jnp.int32, (16, width), 1) // HEAD_DIM
            == lax.broadcasted_iota(jnp.int32, (16, width), 0)
        ).astype(BF16)

        @pl.loop(0, n // step)
        def _(i):
            rows = pl.ds(pl.multiple_of(i * step, step), step)
            columns = scale_ref[0, :, rows].T
            lane = lax.broadcasted_iota(jnp.int32, (step, width), 1)
            scale = columns[:, heads - 1 : heads]
            for h in reversed(range(heads - 1)):
                scale = jnp.where(lane < (h + 1) * HEAD_DIM, columns[:, h : h + 1], scale)
            do = (dot_nn(gb_ref[rows, :], gw_ref[0]) * scale).astype(BF16)
            do_ref[k, rows, :] = do
            prod = do.astype(F32) * o_ref[0, rows, :].astype(F32)
            high = prod.astype(BF16)
            low = (prod - high.astype(F32)).astype(BF16)
            delta_ref[k, :, rows] = dot_nt(pick, high) + dot_nt(pick, low)

        dqt_ref[k] = jnp.zeros(dqt_ref.shape[1:], F32)
        value = dot_nn(gbt_ref[...], o_ref[0]).reshape(Z_DEV, Y_DEV, depth, width)
        for i in range(2):
            @when(8 * i)
            def _():
                stagew_ref[i] = value.astype(BF16)
                start(corew[i])

        @when(4)
        def _():
            recv(corew[0])
            workw_ref[0] = (value + landw_ref[0].astype(F32)).astype(BF16)
            start(segw.y[0])

        @when(9)
        def _():
            workw_ref[1] = value.astype(BF16)

    for bb in range(4):
        @pl.when(b == bb)
        def _():
            first, last = bb * step, (bb + 1) * step
            do = do_ref[k, first:, :]
            q = q_ref[0, first:, :]
            v = v_ref[0, first:last, :]
            lane = lax.broadcasted_iota(jnp.int32, (1, width), 1)
            dk, dv = None, None
            for h in range(heads):
                lanes = head_mask((1, width), h)
                zero = jnp.zeros((), BF16)
                p = p_ref[0, h, :, first:]
                dp = dot_nt(jnp.where(lanes, v, zero), do)
                ds = (p.astype(F32) * (dp - delta_ref[k, h : h + 1, first:])).astype(BF16)
                part = dot_nn(p, do)
                dv = part if dv is None else jnp.where(lane < h * HEAD_DIM, dv, part)
                part = dot_nn(ds, q)
                dk = part if dk is None else jnp.where(lane < h * HEAD_DIM, dk, part)
                head = slice(h * HEAD_DIM, (h + 1) * HEAD_DIM)
                dqt_ref[k, head, first:] += dot_nn(kt_ref[0, head, first:last], ds)
            dk = dk.astype(BF16)
            dv = dv.astype(BF16)
            dq = (dqt_ref[k, :, first:last] * HEAD_DIM ** -0.5).astype(BF16).T
            dqkv_ref[k, first:last, :width] = dq
            dqkv_ref[k, first:last, width : 2 * width] = dk
            dqkv_ref[k, first:last, 2 * width :] = dv
            bqv_ref[mine, 0:1, :] += jnp.sum(dq.astype(F32), 0, keepdims=True)
            bqv_ref[mine, 1:2, :] += jnp.sum(dv.astype(F32), 0, keepdims=True)
            da1_ref[first:last, :] += dot_nt(dqkv_ref[k, first:last, :], gq_ref[0])

    @pl.when((t > 8) & (t % 2 == 1))
    def _():
        rows = pl.ds(pl.multiple_of(b * step, step), step)
        xhat, r = norm_parts(own_ref[rows, :].astype(F32))
        da1 = da1_ref[rows, :]
        sums_ref[0, 0:1, :] += jnp.sum(da1 * xhat, 0, keepdims=True)
        sums_ref[0, 2:3, :] += jnp.sum(da1, 0, keepdims=True)
        dg = da1 * rows_ref[0:1, :]
        dv = r * (
            dg
            - jnp.mean(dg, -1, keepdims=True)
            - xhat * jnp.mean(dg * xhat, -1, keepdims=True)
        )
        own_ref[rows, :] = (dh1_ref[rows, :] + dv).astype(BF16)
        for i in range(4):
            @pl.when(b == i)
            def _():
                out.send(i)

    @pl.when((t == 3) | (t == 7) | (t > 13))
    def _():
        value = dot_nn(a1t_ref[...], dqkv_ref[k]).reshape(Z_DEV, Y_DEV, depth, 3 * width)
        for i in range(2):
            @when(3 + 11 * i)
            def _():
                stage0_ref[i] = value.astype(BF16)
                start(core0[i])

            @when(7 + 8 * i)
            def _():
                recv(core0[i])
                work0_ref[i] = (value + land0_ref[i].astype(F32)).astype(BF16)
                start(seg0.y[i])

    @when(15)
    def _():
        for s in range(4):
            sums_ref[0, 3:5, s * width : (s + 1) * width] = bqv_ref[s, 0:2, :]
        start(sum_core)
        segw.send_x()
        seg2.send_x()
        recv(sum_core)
        sums_ref[1] = sums_ref[0] + sumland_ref[0]
        start(sum_y)
        seg0.fold_y(1)
        recv(sum_y)
        sums_ref[2] = sums_ref[1] + sumland_ref[1]
        start(sum_z)
        out.pass_on(1)
        seg0.send_x()
        recv(sum_z)
        sums_ref[3] = (sums_ref[2] + sumland_ref[2]) + (sumland_ref[3] + sumland_ref[4])
        start(sum_x)
        out.pass_on(2)
        part1_ref[...] = seg1.total()
        part2_ref[...] = seg2.total()
        partw_ref[...] = segw.total()
        layer.finish()
        out.pass_on(3)
        recv(sum_x)
        total_ref[...] = sums_ref[3] + sumland_ref[5]
        part0_ref[...] = seg0.total()
        out.finish()
        links.sent()


def group_and_block(t):
    early = t < 8
    return (
        jnp.where(early, 1 - t // 4, 3 - t % 2),
        jnp.where(early, t % 4, jnp.maximum(t - 8, 0) // 2),
    )


def run_fused_backward(
    tokens, gq, gw, rows, dh1, gb, gbt, q, v, kt, p, scale, o, a1t, layer, fold, work,
    early,
):
    groups, n, _ = tokens.shape
    width = gw.shape[-1]
    heads = width // HEAD_DIM
    hidden = fold.shape[-1]
    depth = D // (Z_DEV * Y_DEV)
    step = n // 4

    def by_group(*shape):
        return pl.BlockSpec(
            (1,) + shape, lambda t: (group_and_block(t)[0],) + (0,) * len(shape)
        )

    p_spec = pl.BlockSpec(
        (1, heads, step, n),
        lambda t: (group_and_block(t)[0], 0, group_and_block(t)[1], 0),
    )

    def early_group(*shape):
        return pl.BlockSpec(
            (1,) + shape, lambda t: (group_and_block(jnp.minimum(t, 9))[0],) + (0,) * len(shape)
        )

    copies = 2 * 12 + 4 + 2 * 15 + 2 * 11 + 6

    def landing(lanes):
        return [
            pltpu.VMEM((2, Z_DEV, depth, lanes), BF16),
            pltpu.VMEM((2, 3, depth, lanes), BF16),
            pltpu.VMEM((depth, lanes), BF16), pltpu.VMEM((depth, lanes), BF16),
        ]

    def working(lanes):
        return [pltpu.VMEM((2, Z_DEV, Y_DEV, depth, lanes), BF16)] * 3

    return pl.pallas_call(
        fused_backward,
        grid=(4 * groups,),
        in_specs=[
            ANY_WHOLE, by_group(D, 3 * width), early_group(D, width), VMEM_WHOLE, VMEM_WHOLE,
            VMEM_WHOLE, VMEM_WHOLE, by_group(n, width), by_group(n, width),
            by_group(width, n), p_spec, early_group(8, n), early_group(n, width),
            VMEM_WHOLE, VMEM_WHOLE, VMEM_WHOLE, VMEM_WHOLE, VMEM_WHOLE,
        ],
        out_specs=[ANY_WHOLE] * 2 + [VMEM_WHOLE] * 5,
        out_shape=[
            shaped(BF16, groups, n, D), shaped(BF16, groups, n, D),
            shaped(F32, depth, 3 * width),
            shaped(F32, depth, width), shaped(F32, depth, hidden),
            shaped(F32, depth, hidden), shaped(F32, 16, D),
        ],
        scratch_shapes=[
            pltpu.VMEM((groups, n, width), BF16),
            pltpu.VMEM((groups, 16, n), F32), pltpu.VMEM((groups, width, n), F32),
            pltpu.VMEM((groups, n, 3 * width), BF16), pltpu.VMEM((n, D), F32),
            pltpu.VMEM((n, D), BF16), pltpu.VMEM((n, D), BF16), pltpu.VMEM((n, D), BF16),
            pltpu.VMEM((groups, 8, width), F32),
        ]
        + landing(hidden)[:1] + landing(hidden) + landing(hidden)
        + working(width) + landing(width)
        + working(3 * width) + landing(3 * width)
        + [
            pltpu.VMEM((4, 16, D), F32), pltpu.VMEM((6, 16, D), F32),
            pltpu.SemaphoreType.DMA((copies,)), pltpu.SemaphoreType.DMA((copies,)),
            pltpu.SemaphoreType.DMA((3,)),
        ],
        compiler_params=pltpu.CompilerParams(
            vmem_limit_bytes=VMEM_LIMIT, collective_id=2, has_side_effects=True
        ),
        name="fused_backward",
    )(tokens, gq, gw, rows, dh1, gb, gbt, q, v, kt, p, scale, o, a1t, layer, fold, work, early)


def place_gradients(
    tie_ref, sums_ref, part0_ref, partw_ref, part1_ref, part2_ref, near_out_ref,
    near_grad_ref, far_out_ref, far_grad_ref, gains_ref, bias_ref, in_ref, out_ref, expand_ref,
    project_ref,
):
    far_out_ref[...] = near_out_ref[...]
    far_grad_ref[...] = near_grad_ref[...]
    own = gains_ref.shape[-1]
    width = partw_ref.shape[-1]

    @pl.when(pl.program_id(0) == 0)
    def _():
        first = (lax.axis_index("dp") * 4 + lax.axis_index("tensor")) * own
        feature = lax.broadcasted_iota(jnp.int32, (D, 128), 0)
        lane = lax.broadcasted_iota(jnp.int32, (D, 128), 1)
        chosen = ((feature == first + lane) & (lane < own)).astype(F32)
        sums = lax.dot_general(
            sums_ref[...], chosen, (((1,), (0,)), ((), ())),
            precision=lax.Precision.HIGHEST, preferred_element_type=F32,
        )[:, :own]
        s0, s1, s2, s3 = tie_ref[0], tie_ref[1], tie_ref[2], tie_ref[3]
        w_out = partw_ref[...].T

        def at(source, wanted, value):
            return jnp.where(source == wanted, value, jnp.zeros_like(value))

        row = lax.broadcasted_iota(jnp.int32, (NSRC, own), 0)
        for i, wanted in enumerate([s0, s0, s0, s1, s2, s3, s2, s2, s2, s2]):
            bias_ref[i] = jnp.where(row == wanted, sums[2 + i : 3 + i], 0.0)
        for s in range(NSRC):
            gains_ref[s, 0:1] = at(s, s0, sums[0:1])
            gains_ref[s, 1:2] = at(s, s2, sums[1:2])
            for j in range(3):
                in_ref[s, j] = at(s, s0, part0_ref[:, j * width : (j + 1) * width])
            out_ref[s] = at(s, s1, w_out)
            expand_ref[s] = at(s, s2, part1_ref[...])
            project_ref[s] = at(s, s3, part2_ref[...])


def run_place_gradients(tie, sums, part0, partw, part1, part2, out, grad, like):
    slots, n, _ = grad.shape
    gains, biases, w_in, w_out, w_expand, w_project = [item.shape for item in like]
    shapes = [
        gains, (biases[1], biases[0], biases[2]), w_in, w_out, w_expand,
        (w_project[0], w_project[2], w_project[1]),
    ]
    out, grad, gains, biases, w_in, w_out, w_expand, w_project = pl.pallas_call(
        place_gradients,
        grid=(slots,),
        in_specs=[SMEM_WHOLE] + [VMEM_WHOLE] * 5
        + [group(n, D), group(n, D)],
        out_specs=[group(n, D), group(n, D)] + [VMEM_WHOLE] * 6,
        out_shape=[shaped(BF16, slots, n, D)] * 2 + [shaped(F32, *item) for item in shapes],
        compiler_params=pltpu.CompilerParams(vmem_limit_bytes=VMEM_LIMIT),
        name="place_gradients",
    )(tie, sums, part0, partw, part1, part2, out, grad)
    biases = biases.transpose(1, 0, 2)
    return out, grad, gains, biases, w_in, w_out, w_expand, w_project.transpose(0, 2, 1)


def plain_step(
    tokens, lengths, tie_map, norm_gains, bias_rows, attention_in, attention_out,
    expand_weight, project_weight, cotangent,
):
    slot_rows = tokens.shape[0] // lengths.shape[0]
    me = lax.axis_index("tensor")
    in_local = lax.dynamic_index_in_dim(attention_in, tie_map[0], 0, keepdims=False)
    out_local = lax.dynamic_index_in_dim(attention_out, tie_map[1], 0, keepdims=False)
    expand_local = lax.dynamic_index_in_dim(expand_weight, tie_map[2], 0, keepdims=False)
    project_local = lax.dynamic_index_in_dim(project_weight, tie_map[3], 0, keepdims=False)
    local0 = jnp.concatenate([in_local, out_local.T[None]], 0)
    row_kinds = jnp.array([0, 0, 0, 1, 2, 3] + [2] * (FF // D), dtype=jnp.int32)
    gain_kinds = jnp.array([0, 2], dtype=jnp.int32)
    gain_pick = norm_gains[tie_map[gain_kinds], jnp.arange(2)]
    bias_pick = bias_rows[tie_map[row_kinds], jnp.arange(row_kinds.shape[0])]
    vectors = jnp.concatenate([gain_pick, bias_pick], 0)
    x = lax.dynamic_slice_in_dim(tokens, me * slot_rows, slot_rows, 0)
    cot = lax.dynamic_slice_in_dim(cotangent, me * slot_rows, slot_rows, 0)
    length = lax.dynamic_slice_in_dim(lengths, me, 1, 0)
    rows = lax.all_gather(vectors, ("dp", "tensor"), axis=1, tiled=True).astype(F32)
    rows = jnp.concatenate([rows, jnp.zeros((4, D), F32)], 0)

    def gathered(piece, axis):
        piece = lax.all_gather(piece, "dp", axis=axis, tiled=True)
        return lax.all_gather(piece, "tensor", axis=0)

    g0 = gathered(local0, 1)
    g1 = gathered(expand_local, 0)
    g2 = gathered(project_local.T, 0)
    groups, width = g0.shape[0], g0.shape[-1]
    bqv = rows[3:5].reshape(2, groups, width).transpose(1, 0, 2)
    q, v, kt, p, o, a1t, h1, a2, a2t = run_attention_forward(length, x, g0, rows, bqv)
    out, d1, d2, dh1, gb, gbt, sums = run_feed_forward(length, cot, a2, a2t, h1, g1, g2, rows)
    d0, xg, sums_in, sums_qv = run_attention_backward(
        x, g0, rows, dh1, gb, gbt, q, v, kt, p, o, a1t
    )
    layer_out = lax.all_gather(out, "tensor", axis=0, tiled=True)
    tokens_grad = lax.all_gather(xg, "tensor", axis=0, tiled=True)

    def scattered(piece, axis):
        piece = lax.psum_scatter(piece, "tensor", scatter_dimension=0)
        return lax.psum_scatter(piece, "dp", scatter_dimension=axis, tiled=True).astype(F32)

    part0 = scattered(d0, 1)
    part1 = scattered(d1, 0)
    part2 = scattered(d2, 0)
    qv = sums_qv[:, :2].transpose(1, 0, 2).reshape(2, D)
    sums = jnp.concatenate(
        [sums_in[0:1], sums[1:2], sums_in[1:2], qv, sums[5:12]], 0
    )
    sums = lax.psum_scatter(sums, ("dp", "tensor"), scatter_dimension=1, tiled=True)
    return layer_out, tokens_grad, *placed(tie_map, sums, part0, part1, part2)


def fused_step(
    tokens, lengths, tie_map, norm_gains, bias_rows, attention_in, attention_out,
    expand_weight, project_weight, cotangent,
):
    slots = lengths.shape[0]
    tokens = tokens.reshape(slots, -1, D)
    cotangent = cotangent.reshape(slots, -1, D)
    gq, gw, g1, g2, rows, q, v, kt, p, scale, o, a1t, h1, a2, a2t = run_fused_forward(
        tie_map, lengths, tokens, norm_gains, bias_rows, attention_in, attention_out,
        expand_weight, project_weight,
    )
    layer, fold, work, dh1, gb, gbt, early = run_fused_feed_forward(
        lengths, cotangent, a2, a2t, h1, g1, g2, rows
    )
    grad, out, part0, partw, part1, part2, sums = run_fused_backward(
        tokens, gq, gw, rows, dh1, gb, gbt, q, v, kt, p, scale, o, a1t, layer, fold,
        work, early,
    )
    out, grad, *placed_grads = run_place_gradients(
        tie_map, sums, part0, partw, part1, part2, out, grad,
        (norm_gains, bias_rows, attention_in, attention_out, expand_weight, project_weight),
    )
    return out.reshape(-1, D), grad.reshape(-1, D), *placed_grads


def placed(tie_map, sums, part0, part1, part2):
    source = jnp.arange(NSRC, dtype=jnp.int32)

    def place(piece, which):
        pick = (source == tie_map[which]).reshape((NSRC,) + (1,) * piece.ndim)
        return jnp.where(pick, piece[None], 0.0)

    def place_rows(piece, kinds):
        pick = source[:, None] == tie_map[jnp.array(kinds, dtype=jnp.int32)][None, :]
        return jnp.where(pick[:, :, None], piece[None], 0.0)

    return (
        place_rows(sums[:2], [0, 2]),
        place_rows(sums[2:], [0, 0, 0, 1, 2, 3] + [2] * (FF // D)),
        place(part0[:3], 0),
        place(part0[3].T, 1),
        place(part1, 2),
        place(part2.T, 3),
    )


def solution(mesh):
    fused = mesh.shape["dp"] == Z_DEV * Y_DEV and mesh.shape["tensor"] == X_DEV * C_DEV
    return jax.shard_map(
        fused_step if fused else plain_step,
        mesh=mesh,
        in_specs=(
            P("dp", None),
            P("dp"),
            P(),
            P(None, None, ("dp", "tensor")),
            P(None, None, ("dp", "tensor")),
            P(None, None, "dp", "tensor"),
            P(None, "tensor", "dp"),
            P(None, "dp", "tensor"),
            P(None, "tensor", "dp"),
            P("dp", None),
        ),
        out_specs=(
            P("dp", None),
            P("dp", None),
            P(None, None, ("dp", "tensor")),
            P(None, None, ("dp", "tensor")),
            P(None, None, "dp", "tensor"),
            P(None, "tensor", "dp"),
            P(None, "dp", "tensor"),
            P(None, "tensor", "dp"),
        ),
        check_vma=False,
    )
```

```python
import jax
import jax.numpy as jnp
from jax import lax
from jax.experimental import pallas as pl
from jax.experimental.pallas import tpu as pltpu
from jax.sharding import PartitionSpec as P

D = 768
HEAD_DIM = 64
FF = 3072
NSRC = 4
EPS = 1e-05
MASKED = -1e30
F32 = jnp.float32
BF16 = jnp.bfloat16
VMEM_LIMIT = 60 * 1024 * 1024


def dot_nn(a, b):
    return lax.dot_general(a, b, (((1,), (0,)), ((), ())), preferred_element_type=F32)


def dot_nt(a, b):
    return lax.dot_general(a, b, (((1,), (1,)), ((), ())), preferred_element_type=F32)


def norm_parts(v):
    center = jnp.mean(v, -1, keepdims=True)
    centered = v - center
    r = lax.rsqrt(jnp.mean(centered * centered, -1, keepdims=True) + EPS)
    return centered * r, r


def head_mask(shape, h):
    lane = lax.broadcasted_iota(jnp.int32, shape, 1)
    return (lane >= h * HEAD_DIM) & (lane < (h + 1) * HEAD_DIM)


def blocks(total, size):
    return [slice(i * size, (i + 1) * size) for i in range(total // size)]


def attention_forward(
    len_ref, x_ref, g_ref, rows_ref, bqv_ref,
    q_ref, v_ref, kt_ref, p_ref, o_ref, a1t_ref, h1_ref, a2_ref, a2t_ref,
    a1_ref, k_ref, vt_ref, ot_ref, attn_ref,
):
    t = pl.program_id(0)
    n = x_ref.shape[0]
    width = g_ref.shape[-1]
    heads = width // HEAD_DIM
    step = 256
    length = len_ref[0]

    @pl.when(t == 0)
    def _():
        @pl.loop(0, n // step)
        def _(b):
            rows = pl.ds(pl.multiple_of(b * step, step), step)
            xhat, _ = norm_parts(x_ref[rows, :].astype(F32))
            a1 = xhat * rows_ref[0:1, :] + rows_ref[2:3, :]
            a1_ref[rows, :] = a1.astype(BF16)
            a1t_ref[:, rows] = a1.astype(BF16).T
            attn_ref[rows, :] = x_ref[rows, :].astype(F32) + rows_ref[5:6, :]

    @pl.loop(0, n // step)
    def _(b):
        rows = pl.ds(pl.multiple_of(b * step, step), step)
        a1 = a1_ref[rows, :]
        q = (dot_nn(a1, g_ref[0, 0]) + bqv_ref[0, 0:1, :]).astype(BF16)
        q_ref[0, rows, :] = q * jnp.asarray(HEAD_DIM ** -0.5, BF16)
        k = dot_nn(a1, g_ref[0, 1]).astype(BF16)
        k_ref[rows, :] = k
        kt_ref[0, :, rows] = k.T
        v = (dot_nn(a1, g_ref[0, 2]) + bqv_ref[0, 1:2, :]).astype(BF16)
        v_ref[0, rows, :] = v
        vt_ref[:, rows] = v.T

    for h in range(heads):
        k = k_ref[...]
        k = jnp.where(head_mask(k.shape, h), k, jnp.zeros_like(k))
        for b in range(n // step):
            first, last = b * step, (b + 1) * step
            q = q_ref[0, first:last, :]
            key = lax.broadcasted_iota(jnp.int32, (last, step), 0)
            query = lax.broadcasted_iota(jnp.int32, (step, step), 1) + first
            s = dot_nt(k[:last], q)
            near = jnp.where(
                (key[first:] <= query) & (key[first:] < length), s[first:], MASKED
            )
            if b:
                far = jnp.where(key[:first] < length, s[:first], MASKED)
                top = jnp.maximum(
                    jnp.max(far, 0, keepdims=True), jnp.max(near, 0, keepdims=True)
                )
                e_far = jnp.exp(far - top)
                e_near = jnp.exp(near - top)
                total = jnp.sum(e_far, 0, keepdims=True) + jnp.sum(e_near, 0, keepdims=True)
                scale = 1.0 / total
                p_ref[0, h, :first, first:last] = (e_far * scale).astype(BF16)
            else:
                top = jnp.max(near, 0, keepdims=True)
                e_near = jnp.exp(near - top)
                scale = 1.0 / jnp.sum(e_near, 0, keepdims=True)
            p_ref[0, h, first:last, first:last] = (e_near * scale).astype(BF16)
            ot_ref[h * HEAD_DIM : (h + 1) * HEAD_DIM, first:last] = dot_nn(
                vt_ref[h * HEAD_DIM : (h + 1) * HEAD_DIM, :last],
                p_ref[0, h, :last, first:last],
            ).astype(BF16)

    @pl.loop(0, n // step)
    def _(b):
        rows = pl.ds(pl.multiple_of(b * step, step), step)
        o = ot_ref[:, rows].T
        o_ref[0, rows, :] = o
        attn_ref[rows, :] += dot_nt(o, g_ref[0, 3])

    @pl.when(t == pl.num_programs(0) - 1)
    def _():
        @pl.loop(0, n // step)
        def _(b):
            rows = pl.ds(pl.multiple_of(b * step, step), step)
            h1 = attn_ref[rows, :]
            h1_ref[rows, :] = h1
            xhat, _ = norm_parts(h1)
            a2 = (xhat * rows_ref[1:2, :] + rows_ref[6:7, :]).astype(BF16)
            a2_ref[rows, :] = a2
            a2t_ref[:, rows] = a2.T


SQRT_2_PI = 0.7978845608028654


def feed_forward_both(
    len_ref, c_ref, a2_ref, a2t_ref, h1_ref, w1_ref, w2_ref, rows_ref,
    out_ref, d1_ref, d2_ref, dh1_ref, gb_ref, gbt_ref, sums_ref,
    gf_ref, gft_ref, feed_ref, da2_ref, h_ref, df_ref,
):
    t = pl.program_id(0)
    n = c_ref.shape[0]
    step = 256
    length = len_ref[0]

    @pl.when(t == 0)
    def _():
        sums_ref[...] = jnp.zeros_like(sums_ref)

        @pl.loop(0, n // step)
        def _(b):
            rows = pl.ds(pl.multiple_of(b * step, step), step)
            place = b * step + lax.broadcasted_iota(jnp.int32, (step, 1), 0)
            live = (place < length).astype(F32)
            g = (c_ref[rows, :].astype(F32) * live).astype(BF16)
            gf_ref[rows, :] = g
            gft_ref[:, rows] = g.T
            sums_ref[7:8, :] += jnp.sum(g.astype(F32), 0, keepdims=True)

    bias = rows_ref[pl.ds(8 + t, 1), :]

    @pl.loop(0, n // step)
    def _(b):
        rows = pl.ds(pl.multiple_of(b * step, step), step)
        f = dot_nn(a2_ref[rows, :], w1_ref[0]) + bias
        dh = dot_nn(gf_ref[rows, :], w2_ref[0])
        f2 = f * f
        th = jnp.tanh(f * (SQRT_2_PI + (SQRT_2_PI * 0.044715) * f2))
        half = 0.5 + 0.5 * th
        h = (f * half).astype(BF16)
        slope = half + f * (0.5 - 0.5 * th * th) * (
            SQRT_2_PI + (3 * SQRT_2_PI * 0.044715) * f2
        )
        df = (dh * slope).astype(BF16)
        h_ref[rows, :] = h
        df_ref[rows, :] = df
        sums_ref[pl.ds(8 + t, 1), :] += jnp.sum(df.astype(F32), 0, keepdims=True)
        feed = dot_nt(h, w2_ref[0])
        da2 = dot_nt(df, w1_ref[0])

        @pl.when(t == 0)
        def _():
            feed_ref[rows, :] = feed
            da2_ref[rows, :] = da2

        @pl.when(t > 0)
        def _():
            feed_ref[rows, :] += feed
            da2_ref[rows, :] += da2

    @pl.loop(0, D // step)
    def _(b):
        rows = pl.ds(pl.multiple_of(b * step, step), step)
        d1_ref[0, rows, :] = dot_nn(a2t_ref[rows, :], df_ref[...]).astype(BF16)
        d2_ref[0, rows, :] = dot_nn(gft_ref[rows, :], h_ref[...]).astype(BF16)

    @pl.when(t == pl.num_programs(0) - 1)
    def _():
        @pl.loop(0, n // step)
        def _(b):
            rows = pl.ds(pl.multiple_of(b * step, step), step)
            place = b * step + lax.broadcasted_iota(jnp.int32, (step, 1), 0)
            live = (place < length).astype(F32)
            h1 = h1_ref[rows, :]
            out_ref[rows, :] = (live * (h1 + (feed_ref[rows, :] + rows_ref[7:8, :]))).astype(BF16)
            xhat, r = norm_parts(h1)
            da2 = da2_ref[rows, :]
            sums_ref[1:2, :] += jnp.sum(da2 * xhat, 0, keepdims=True)
            sums_ref[6:7, :] += jnp.sum(da2, 0, keepdims=True)
            dg = da2 * rows_ref[1:2, :]
            dv = r * (
                dg
                - jnp.mean(dg, -1, keepdims=True)
                - xhat * jnp.mean(dg * xhat, -1, keepdims=True)
            )
            dh1 = live * c_ref[rows, :].astype(F32) + dv
            dh1_ref[rows, :] = dh1
            gb = dh1.astype(BF16)
            gb_ref[rows, :] = gb
            gbt_ref[:, rows] = gb.T
            sums_ref[5:6, :] += jnp.sum(gb.astype(F32), 0, keepdims=True)


def attention_backward(
    x_ref, g_ref, rows_ref, dh1_ref, gb_ref, gbt_ref, q_ref, v_ref, kt_ref, p_ref,
    o_ref, a1t_ref,
    d0_ref, xg_ref, sums_ref, bqv_ref,
    do_ref, delta_ref, dqt_ref, dq_ref, dk_ref, dv_ref, da1_ref,
):
    t = pl.program_id(0)
    n = x_ref.shape[0]
    width = g_ref.shape[-1]
    heads = width // HEAD_DIM
    step = 256
    pick = (
        lax.broadcasted_iota(jnp.int32, (16, width), 1) // HEAD_DIM
        == lax.broadcasted_iota(jnp.int32, (16, width), 0)
    ).astype(BF16)

    @pl.loop(0, n // step)
    def _(b):
        rows = pl.ds(pl.multiple_of(b * step, step), step)
        do = dot_nn(gb_ref[rows, :], g_ref[0, 3]).astype(BF16)
        do_ref[rows, :] = do
        prod = do.astype(F32) * o_ref[0, rows, :].astype(F32)
        high = prod.astype(BF16)
        low = (prod - high.astype(F32)).astype(BF16)
        delta_ref[:, rows] = dot_nt(pick, high) + dot_nt(pick, low)

    dqt_ref[...] = jnp.zeros_like(dqt_ref)
    for b in range(n // step):
        first, last = b * step, (b + 1) * step
        do = do_ref[first:, :]
        q = q_ref[0, first:, :]
        v = v_ref[0, first:last, :]
        dk, dv = None, None
        for h in range(heads):
            mine = head_mask((1, width), h)
            zero = jnp.zeros((), BF16)
            p = p_ref[0, h, first:last, first:]
            dp = dot_nt(jnp.where(mine, v, zero), do)
            ds = (p.astype(F32) * (dp - delta_ref[h : h + 1, first:])).astype(BF16)
            part = dot_nn(p, jnp.where(mine, do, zero))
            dv = part if dv is None else dv + part
            part = dot_nn(ds, jnp.where(mine, q, zero))
            dk = part if dk is None else dk + part
            head = slice(h * HEAD_DIM, (h + 1) * HEAD_DIM)
            dqt_ref[head, first:] += dot_nn(kt_ref[0, head, first:last], ds)
        dk_ref[first:last, :] = dk.astype(BF16)
        dv_ref[first:last, :] = dv.astype(BF16)

    @pl.when(t == 0)
    def _():
        da1_ref[...] = jnp.zeros_like(da1_ref)

    bqv_ref[...] = jnp.zeros_like(bqv_ref)

    @pl.loop(0, n // step)
    def _(b):
        rows = pl.ds(pl.multiple_of(b * step, step), step)
        dq = (dqt_ref[:, rows] * HEAD_DIM ** -0.5).astype(BF16).T
        dk = dk_ref[rows, :]
        dv = dv_ref[rows, :]
        dq_ref[rows, :] = dq
        bqv_ref[0, 0:1, :] += jnp.sum(dq.astype(F32), 0, keepdims=True)
        bqv_ref[0, 1:2, :] += jnp.sum(dv.astype(F32), 0, keepdims=True)
        da1_ref[rows, :] += (
            dot_nt(dq, g_ref[0, 0]) + dot_nt(dk, g_ref[0, 1]) + dot_nt(dv, g_ref[0, 2])
        )

    @pl.loop(0, D // step)
    def _(b):
        rows = pl.ds(pl.multiple_of(b * step, step), step)
        a1t = a1t_ref[rows, :]
        d0_ref[0, 0, rows, :] = dot_nn(a1t, dq_ref[...]).astype(BF16)
        d0_ref[0, 1, rows, :] = dot_nn(a1t, dk_ref[...]).astype(BF16)
        d0_ref[0, 2, rows, :] = dot_nn(a1t, dv_ref[...]).astype(BF16)
        d0_ref[0, 3, rows, :] = dot_nn(gbt_ref[rows, :], o_ref[0]).astype(BF16)

    @pl.when(t == pl.num_programs(0) - 1)
    def _():
        sums_ref[...] = jnp.zeros_like(sums_ref)

        @pl.loop(0, n // step)
        def _(b):
            rows = pl.ds(pl.multiple_of(b * step, step), step)
            xhat, r = norm_parts(x_ref[rows, :].astype(F32))
            da1 = da1_ref[rows, :]
            sums_ref[0:1, :] += jnp.sum(da1 * xhat, 0, keepdims=True)
            sums_ref[1:2, :] += jnp.sum(da1, 0, keepdims=True)
            dg = da1 * rows_ref[0:1, :]
            dv = r * (
                dg
                - jnp.mean(dg, -1, keepdims=True)
                - xhat * jnp.mean(dg * xhat, -1, keepdims=True)
            )
            xg_ref[rows, :] = (dh1_ref[rows, :] + dv).astype(BF16)


def whole(*shape):
    return pl.BlockSpec(shape, lambda t: (0,) * len(shape))


def group(*shape):
    return pl.BlockSpec((1,) + shape, lambda t: (t,) + (0,) * len(shape))


def shaped(dtype, *shape):
    return jax.ShapeDtypeStruct(shape, dtype)


SMEM_WHOLE = pl.BlockSpec(memory_space=pltpu.SMEM)


def run_attention_forward(length, x, g0, rows, bqv):
    n = x.shape[0]
    groups, _, _, width = g0.shape
    heads = width // HEAD_DIM
    return pl.pallas_call(
        attention_forward,
        grid=(groups,),
        in_specs=[SMEM_WHOLE, whole(n, D), group(4, D, width), whole(16, D), group(2, width)],
        out_specs=[
            group(n, width), group(n, width), group(width, n), group(heads, n, n),
            group(n, width), whole(D, n), whole(n, D), whole(n, D), whole(D, n),
        ],
        out_shape=[
            shaped(BF16, groups, n, width), shaped(BF16, groups, n, width),
            shaped(BF16, groups, width, n), shaped(BF16, groups, heads, n, n),
            shaped(BF16, groups, n, width), shaped(BF16, D, n), shaped(F32, n, D),
            shaped(BF16, n, D), shaped(BF16, D, n),
        ],
        scratch_shapes=[
            pltpu.VMEM((n, D), BF16), pltpu.VMEM((n, width), BF16),
            pltpu.VMEM((width, n), BF16), pltpu.VMEM((width, n), BF16),
            pltpu.VMEM((n, D), F32),
        ],
        compiler_params=pltpu.CompilerParams(vmem_limit_bytes=VMEM_LIMIT),
        name="attention_forward",
    )(length, x, g0, rows, bqv)


def run_feed_forward(length, cot, a2, a2t, h1, g1, g2, rows):
    n = cot.shape[0]
    groups, _, width = g1.shape
    return pl.pallas_call(
        feed_forward_both,
        grid=(groups,),
        in_specs=[
            SMEM_WHOLE, whole(n, D), whole(n, D), whole(D, n), whole(n, D),
            group(D, width), group(D, width), whole(16, D),
        ],
        out_specs=[
            whole(n, D), group(D, width), group(D, width), whole(n, D), whole(n, D),
            whole(D, n), whole(16, D),
        ],
        out_shape=[
            shaped(BF16, n, D), shaped(BF16, groups, D, width), shaped(BF16, groups, D, width),
            shaped(F32, n, D), shaped(BF16, n, D), shaped(BF16, D, n), shaped(F32, 16, D),
        ],
        scratch_shapes=[
            pltpu.VMEM((n, D), BF16), pltpu.VMEM((D, n), BF16), pltpu.VMEM((n, D), F32),
            pltpu.VMEM((n, D), F32), pltpu.VMEM((n, width), BF16), pltpu.VMEM((n, width), BF16),
        ],
        compiler_params=pltpu.CompilerParams(vmem_limit_bytes=VMEM_LIMIT),
        name="feed_forward_both",
    )(length, cot, a2, a2t, h1, g1, g2, rows)


def run_attention_backward(x, g0, rows, dh1, gb, gbt, q, v, kt, p, o, a1t):
    n = x.shape[0]
    groups, _, _, width = g0.shape
    heads = width // HEAD_DIM
    return pl.pallas_call(
        attention_backward,
        grid=(groups,),
        in_specs=[
            whole(n, D), group(4, D, width), whole(16, D), whole(n, D), whole(n, D),
            whole(D, n), group(n, width), group(n, width), group(width, n),
            group(heads, n, n), group(n, width), whole(D, n),
        ],
        out_specs=[group(4, D, width), whole(n, D), whole(8, D), group(8, width)],
        out_shape=[
            shaped(BF16, groups, 4, D, width), shaped(BF16, n, D), shaped(F32, 8, D),
            shaped(F32, groups, 8, width),
        ],
        scratch_shapes=[
            pltpu.VMEM((n, width), BF16), pltpu.VMEM((16, n), F32), pltpu.VMEM((width, n), F32),
            pltpu.VMEM((n, width), BF16), pltpu.VMEM((n, width), BF16),
            pltpu.VMEM((n, width), BF16), pltpu.VMEM((n, D), F32),
        ],
        compiler_params=pltpu.CompilerParams(vmem_limit_bytes=VMEM_LIMIT),
        name="attention_backward",
    )(x, g0, rows, dh1, gb, gbt, q, v, kt, p, o, a1t)


Z_DEV, Y_DEV, X_DEV, C_DEV = 4, 2, 2, 2


class Place:
    def __init__(self):
        dp, self.t = lax.axis_index("dp"), lax.axis_index("tensor")
        self.dp = dp
        self.z, self.y = dp // 2, dp % 2
        self.x, self.c = self.t // 2, self.t % 2
        self.other_y = 1 - self.y
        self.zs = [
            self.z,
            self.z + 1 - 2 * (self.z % 2),
            self.z + 2 - 4 * (self.z // 2),
            3 - self.z,
        ]
        self.ts = [
            self.t,
            self.t + 1 - 2 * (self.t % 2),
            self.t + 2 - 4 * (self.t // 2),
            3 - self.t,
        ]
        self.to_z = [dict(dp=z * 2 + self.y) for z in self.zs]
        self.to_y = dict(dp=self.z * 2 + self.other_y)
        self.to_x = dict(tensor=self.ts[2])
        self.to_core = dict(tensor=self.ts[1])

    def group(self, k):
        return lax.select(
            k == 0, self.ts[0],
            lax.select(k == 1, self.ts[1], lax.select(k == 2, self.ts[2], self.ts[3])),
        )

    def greet(self):
        barrier = pltpu.get_barrier_semaphore()
        others = self.to_z[1:] + [self.to_y, self.to_x, self.to_core]
        for device in others:
            pl.semaphore_signal(
                barrier, inc=1, device_id=device, device_id_type=pl.DeviceIdType.MESH
            )
        pl.semaphore_wait(barrier, len(others))


class Links:
    def __init__(self, send_sem, recv_sem):
        self.send_sem, self.recv_sem = send_sem, recv_sem
        self.copies = []

    def add(self, device, src, dst):
        number = len(self.copies)
        copy = pltpu.make_async_remote_copy(
            src_ref=src,
            dst_ref=dst,
            send_sem=self.send_sem.at[number],
            recv_sem=self.recv_sem.at[number],
            device_id=device,
            device_id_type=pl.DeviceIdType.MESH,
        )
        self.copies.append(copy)
        return copy

    def sent(self, *apart):
        for copy in self.copies:
            if all(copy is not other for other in apart):
                copy.wait_send()


def flat(copies):
    for item in copies:
        if isinstance(item, list):
            yield from flat(item)
        else:
            yield item


def start(*copies):
    for copy in flat(copies):
        copy.start()


def recv(*copies):
    for copy in flat(copies):
        copy.wait_recv()


class Gather:
    def __init__(self, links, place, own, full, x_first, single=True, last=True):
        every = slice(None)
        y, other = place.y, place.other_y

        def same(device, k, yy, to):
            return links.add(device, full(k, every, yy), full(to, every, yy))

        if x_first:
            self.first = [links.add(place.to_x, own, full(2, place.z, y))]

        def along_z(k, block):
            passed = full(k, place.zs[2], y)
            return [
                links.add(place.to_z[1], block, full(k, place.z, y)),
                links.add(place.to_z[2], block, full(k, place.z, y)),
                links.add(place.to_z[1], passed, passed),
            ]

        self.z = along_z(0, own)
        if x_first:
            self.far = along_z(2, full(2, place.z, y))
            self.second = [same(place.to_y, 0, y, 0)]
            if last:
                self.second.append(same(place.to_y, 2, y, 2))
            blocks = [(0, y), (2, y), (0, other), (2, other)]
        else:
            if single:
                self.first = [same(place.to_y, 0, y, 0)]
            else:
                self.first = [links.add(place.to_y, own, full(0, place.z, y))]
                for k in range(1, 4):
                    block = full(0, place.zs[k], y)
                    self.first.append(links.add(place.to_y, block, block))
            self.second = [same(place.to_x, 0, y, 2)]
            if last:
                self.second.append(same(place.to_x, 0, other, 2))
            blocks = [(0, y), (0, other), (2, y), (2, other)]
        blocks = blocks if last else blocks[:-1]
        self.core = [same(place.to_core, k, yy, k + 1) for k, yy in blocks]


def fused_forward(
    tie_ref, len_ref, tokens_ref, gains_ref, bias_ref, in_ref, out_ref, expand_ref,
    project_ref,
    gqt_ref, gw_ref, flat1_ref, flat2_ref, rows_ref,
    q_ref, v_ref, kt_ref, p_ref, scale_ref, o_ref, ot_ref, a1t_ref, h1_ref, a2_ref, a2t_ref,
    own0_ref, ownw_ref, own1_ref, own2_ref, square_ref, vec_ref,
    all0_ref, allw_ref, w1_ref, w2_ref, vecs_ref, bqv_ref, x_ref, a1_ref, k_ref, qt_ref, vt_ref,
    send_sem, recv_sem, local_sem,
):
    t = pl.program_id(0)
    n, _ = x_ref.shape
    width = allw_ref.shape[-1]
    heads = width // HEAD_DIM
    step = 256
    place = Place()
    length = len_ref[place.t]
    links = Links(send_sem, recv_sem)
    z, y, x, c = place.z, place.y, place.x, place.c
    vec_z = [
        links.add(place.to_z[k], vec_ref, vecs_ref.at[z, y, x, c]) for k in range(1, 4)
    ]
    vec_y = links.add(place.to_y, vecs_ref.at[:, y, x, c], vecs_ref.at[:, y, x, c])
    vec_x = links.add(place.to_x, vecs_ref.at[:, :, x, c], vecs_ref.at[:, :, x, c])
    vec_core = links.add(place.to_core, vecs_ref.at[:, :, :, c], vecs_ref.at[:, :, :, c])
    seg0 = Gather(
        links, place, own0_ref, lambda k, z, y: all0_ref.at[k, z, y], False, False
    )
    segw = Gather(links, place, ownw_ref, lambda k, z, y: allw_ref.at[k, z, y], False)
    seg1 = Gather(
        links, place, own1_ref, lambda k, z, y: w1_ref.at[k, z, y], False, last=False
    )
    seg2 = Gather(
        links, place, own2_ref, lambda k, z, y: w2_ref.at[k, z, y], True, last=False
    )
    flush = [
        pltpu.make_async_copy(w1_ref, flat1_ref, local_sem.at[0]),
        pltpu.make_async_copy(w2_ref, flat2_ref, local_sem.at[1]),
    ]
    fetch = pltpu.make_async_copy(tokens_ref.at[place.t], x_ref, local_sem.at[2])

    def begin_z(*copies):
        for near, far, _ in copies:
            start(far)
        for near, far, _ in copies:
            start(near)

    def relay_z(copies):
        recv(copies[1])
        start(copies[2])

    def pass_on(seg, stage):
        if stage == 0:
            recv(seg.z[0], seg.z[2])
            start(seg.first, seg.second[0], seg.core[0])
        elif stage == 1:
            recv(seg.first)
            start(seg.second[1:], seg.core[1])
        else:
            recv(seg.second[stage - 2])
            start(seg.core[stage])

    @pl.when(t == 0)
    def _():
        s0, s1, s2, s3 = tie_ref[0], tie_ref[1], tie_ref[2], tie_ref[3]
        fetch.start()
        square_ref[...] = jnp.zeros_like(square_ref)
        gain = gains_ref.shape[-1]
        square_ref[0:1, :gain] = gains_ref[s0].astype(F32)[0:1]
        square_ref[1:2, :gain] = gains_ref[s2].astype(F32)[1:2]
        kinds = [s0, s0, s0, s1, s2, s3, s2, s2, s2, s2]
        for i, source in enumerate(kinds):
            wide = bias_ref[i].astype(F32)
            here = lax.broadcasted_iota(jnp.int32, wide.shape, 0) == source
            square_ref[2 + i : 3 + i, :gain] = jnp.sum(
                jnp.where(here, wide, 0.0), 0, keepdims=True
            )
        vec_ref[...] = square_ref[...].T[:gain]
        for j in range(3):
            own0_ref[:, j * width : (j + 1) * width] = in_ref[s0, j]
        place.greet()
        start(vec_z)
        begin_z(seg0.z)
        start(seg0.first[0])
        vecs_ref[z, y, x, c] = vec_ref[...]
        ones = lax.broadcasted_iota(jnp.int32, (vt_ref.shape[1] - HEAD_DIM, n), 0) == 0
        for h in range(heads):
            vt_ref[h, HEAD_DIM:, :] = ones.astype(BF16)
        all0_ref[0, z, y] = own0_ref[...]
        ownw_ref[...] = out_ref[s1].T
        allw_ref[0, z, y] = ownw_ref[...]
        own1_ref[...] = expand_ref[s2]
        own2_ref[...] = project_ref[s3]
        w1_ref[0, z, y] = own1_ref[...]
        w2_ref[0, z, y] = own2_ref[...]
        recv(vec_z)
        start(vec_y)
        relay_z(seg0.z)
        start(seg0.first[2])
        recv(seg0.z[0])
        start(seg0.first[1])
        recv(vec_y)
        start(vec_x)
        begin_z(segw.z, seg1.z, seg2.z)
        start(seg2.first)
        recv(vec_x)
        start(vec_core)
        recv(vec_core)
        vecs = vecs_ref[...].reshape(D, vecs_ref.shape[-1]).T[:16]
        rows_ref[...] = vecs
        for k in range(4):
            part = slice(k * width, (k + 1) * width)
            bqv_ref[k, 0:1, :width] = vecs[3:4, part]
            bqv_ref[k, 0:1, width : 2 * width] = jnp.zeros((1, width), F32)
            bqv_ref[k, 0:1, 2 * width :] = vecs[4:5, part]
        fetch.wait()

        @pl.loop(0, n // step)
        def _(b):
            rows = pl.ds(pl.multiple_of(b * step, step), step)
            wide = x_ref[rows, :].astype(F32)
            xhat, _ = norm_parts(wide)
            a1 = (xhat * rows_ref[0:1, :] + rows_ref[2:3, :]).astype(BF16)
            a1_ref[rows, :] = a1
            a1t_ref[:, rows] = a1.T
            h1_ref[rows, :] = wide + rows_ref[5:6, :]

        recv(seg0.z[2])
        start(seg0.first[3], seg0.second[0], seg0.core[0])
        relay_z(segw.z)
        recv(seg0.first)
        start(seg0.second[1], seg0.core[1])

    @pl.when(t == 1)
    def _():
        recv(seg0.core[0], seg0.core[1])

    @pl.when(t == 2)
    def _():
        recv(seg2.z[0], seg2.z[2])
        start(seg2.second[0], seg2.core[0])
        relay_z(seg2.far)
        pass_on(segw, 3)

    @pl.when(t == 3)
    def _():
        recv(seg0.core[2], seg0.core[3])
        pass_on(seg1, 2)
        recv(seg2.far[0], seg2.far[2])
        start(seg2.core[1])
        pass_on(seg2, 2)

    gq = all0_ref[t].reshape(D, 3 * width)
    gqt_ref[0] = gq.T
    mine = place.group(t)
    qkv = dot_nn(a1_ref[...], gq) + bqv_ref[mine, 0:1, :]
    q = qkv[:, :width].astype(BF16) * jnp.asarray(HEAD_DIM ** -0.5, BF16)
    k = qkv[:, width : 2 * width].astype(BF16)
    v = qkv[:, 2 * width :].astype(BF16)
    q_ref[0] = q
    kt_ref[0] = k.T
    v_ref[0] = v
    vt = v.T
    for h in range(heads):
        vt_ref[h, :HEAD_DIM, :] = vt[h * HEAD_DIM : (h + 1) * HEAD_DIM]
    spare = k_ref.shape[1] - width
    dead = lax.broadcasted_iota(jnp.int32, (n, spare), 0) >= length
    first_column = lax.broadcasted_iota(jnp.int32, (n, spare), 1) == 0
    first_row = lax.broadcasted_iota(jnp.int32, (spare, n), 0) == 0
    k_ref[:, :width] = k
    k_ref[:, width:] = jnp.where(first_column & dead, MASKED, 0.0).astype(BF16)
    qt_ref[:width, :] = q.T
    qt_ref[width:, :] = jnp.where(first_row, 1.0, 0.0).astype(BF16)

    @pl.when(t == 0)
    def _():
        pass_on(segw, 0)
        relay_z(seg1.z)
        relay_z(seg2.z)

    units = [(h, b) for h in range(heads) for b in range(n // step)]

    def scores(h, b):
        first, last = b * step, (b + 1) * step
        qt = qt_ref[:, first:last]
        row = lax.broadcasted_iota(jnp.int32, (qt.shape[0], 1), 0)
        keep = ((row >= h * HEAD_DIM) & (row < (h + 1) * HEAD_DIM)) | (row >= width)
        return dot_nn(k_ref[:last, :], jnp.where(keep, qt, jnp.zeros((), BF16)))

    def attend(h, b, s):
        first, last = b * step, (b + 1) * step
        key = lax.broadcasted_iota(jnp.int32, (step, step), 0)
        query = lax.broadcasted_iota(jnp.int32, (step, step), 1)
        near = jnp.where(key <= query, s[first:], MASKED)
        top = jnp.max(near, 0, keepdims=True)
        if b:
            far = s[:first]
            top = jnp.maximum(top, jnp.max(far, 0, keepdims=True))
        e_near = jnp.exp((near - top).astype(BF16))
        p_ref[0, h, first:last, first:last] = e_near
        o = dot_nn(vt_ref[h, :, first:last], e_near)
        if b:
            e_far = jnp.exp((far - top).astype(BF16))
            p_ref[0, h, :first, first:last] = e_far
            o += dot_nn(vt_ref[h, :, :first], e_far)
        scale = 1.0 / o[HEAD_DIM : HEAD_DIM + 1]
        scale_ref[0, h : h + 1, first:last] = scale
        ot_ref[0, h * HEAD_DIM : (h + 1) * HEAD_DIM, first:last] = (
            o[:HEAD_DIM] * scale
        ).astype(BF16)

    scale_ref[0, heads:, :] = jnp.zeros((scale_ref.shape[1] - heads, n), F32)
    s = scores(*units[0])
    for i, unit in enumerate(units):
        ahead = scores(*units[i + 1]) if i + 1 < len(units) else None
        attend(*unit, s)
        s = ahead

    @pl.when(t == 0)
    def _():
        pass_on(seg0, 2)
        pass_on(segw, 1)
        pass_on(seg1, 0)

    @pl.when(t == 1)
    def _():
        pass_on(seg0, 3)
        recv(seg2.first)
        begin_z(seg2.far)
        pass_on(seg1, 1)
        recv(segw.core[0], segw.core[1])

    @pl.when(t == 2)
    def _():
        pass_on(segw, 2)

    @pl.when(t == 3)
    def _():
        recv(segw.core[2], segw.core[3])

    gw_ref[0] = allw_ref[t].reshape(gw_ref.shape[1:])
    o = ot_ref[0].T
    o_ref[0] = o
    h1_ref[...] += dot_nt(o, gw_ref[0])

    @pl.when(t == 3)
    def _():
        @pl.loop(0, n // step)
        def _(b):
            rows = pl.ds(pl.multiple_of(b * step, step), step)
            h1 = h1_ref[rows, :]
            xhat, _ = norm_parts(h1)
            a2 = (xhat * rows_ref[1:2, :] + rows_ref[6:7, :]).astype(BF16)
            a2_ref[rows, :] = a2
            a2t_ref[:, rows] = a2.T

        recv(seg1.core)
        flush[0].start()
        recv(seg2.core)
        flush[1].start()
        links.sent()
        for copy in flush:
            copy.wait()


N_GATHER = 6 + 13 + 10 + 8 + 11
VMEM_WHOLE = pl.BlockSpec(memory_space=pltpu.VMEM)
ANY_WHOLE = pl.BlockSpec(memory_space=pl.ANY)


def run_fused_forward(tie, lengths, tokens, gains, biases, w_in, w_out, w_expand, w_project):
    groups, n, _ = tokens.shape
    depth, width = w_in.shape[-2:]
    heads = width // HEAD_DIM
    hidden = w_expand.shape[-1]
    w_project = w_project.transpose(0, 2, 1)
    biases = biases.transpose(1, 0, 2)
    own = gains.shape[-1]
    return pl.pallas_call(
        fused_forward,
        grid=(groups,),
        in_specs=[SMEM_WHOLE, SMEM_WHOLE, ANY_WHOLE] + [VMEM_WHOLE] * 6,
        out_specs=[
            group(3 * width, D), group(D, width), ANY_WHOLE, ANY_WHOLE, VMEM_WHOLE,
            group(n, width), group(n, width), group(width, n), group(heads, n, n),
            group(8, n), group(n, width), group(width, n), VMEM_WHOLE, VMEM_WHOLE, VMEM_WHOLE, VMEM_WHOLE,
        ],
        out_shape=[
            shaped(BF16, groups, 3 * width, D), shaped(BF16, groups, D, width),
            shaped(BF16, groups, Z_DEV, Y_DEV, depth, hidden),
            shaped(BF16, groups, Z_DEV, Y_DEV, depth, hidden),
            shaped(F32, 16, D),
            shaped(BF16, groups, n, width), shaped(BF16, groups, n, width),
            shaped(BF16, groups, width, n), shaped(BF16, groups, heads, n, n),
            shaped(F32, groups, 8, n), shaped(BF16, groups, n, width),
            shaped(BF16, groups, width, n), shaped(BF16, D, n), shaped(F32, n, D),
            shaped(BF16, n, D), shaped(BF16, D, n),
        ],
        scratch_shapes=[
            pltpu.VMEM((depth, 3 * width), BF16), pltpu.VMEM((depth, width), BF16),
            pltpu.VMEM((depth, hidden), BF16), pltpu.VMEM((depth, hidden), BF16),
            pltpu.VMEM((128, 128), F32), pltpu.VMEM((own, 128), F32),
            pltpu.VMEM((groups, Z_DEV, Y_DEV, depth, 3 * width), BF16),
            pltpu.VMEM((groups, Z_DEV, Y_DEV, depth, width), BF16),
            pltpu.VMEM((groups, Z_DEV, Y_DEV, depth, hidden), BF16),
            pltpu.VMEM((groups, Z_DEV, Y_DEV, depth, hidden), BF16),
            pltpu.VMEM((Z_DEV, Y_DEV, X_DEV, C_DEV, own, 128), F32),
            pltpu.VMEM((groups, 8, 3 * width), F32),
            pltpu.VMEM((n, D), BF16), pltpu.VMEM((n, D), BF16), pltpu.VMEM((n, 256), BF16),
            pltpu.VMEM((256, n), BF16), pltpu.VMEM((heads, HEAD_DIM + 16, n), BF16),
            pltpu.SemaphoreType.DMA((N_GATHER,)), pltpu.SemaphoreType.DMA((N_GATHER,)),
            pltpu.SemaphoreType.DMA((3,)),
        ],
        compiler_params=pltpu.CompilerParams(
            vmem_limit_bytes=VMEM_LIMIT, collective_id=0, has_side_effects=True
        ),
        name="fused_forward",
    )(tie, lengths, tokens, gains, biases, w_in, w_out, w_expand, w_project)


class Result:
    def __init__(self, links, place, own_ref, passing_ref, out_ref, step, sem):
        count = own_ref.shape[0] // step
        self.own_ref, self.passing_ref, self.out_ref, self.sem = own_ref, passing_ref, out_ref, sem
        self.place = place
        self.x, self.core, self.far = [], [], []
        for i in range(count):
            rows = pl.ds(i * step, step)
            mine, theirs = out_ref.at[place.t, rows], out_ref.at[place.ts[2], rows]
            self.x.append(links.add(place.to_x, own_ref.at[rows], passing_ref.at[rows]))
            self.core.append(links.add(place.to_core, own_ref.at[rows], mine))
            self.far.append(links.add(place.to_core, passing_ref.at[rows], theirs))

    def send(self, i):
        start(self.x[i], self.core[i])

    def pass_on(self, i):
        recv(self.x[i])
        start(self.far[i])

    def finish(self):
        for ref, where in [
            (self.own_ref, self.place.t), (self.passing_ref, self.place.ts[2])
        ]:
            copy = pltpu.make_async_copy(ref, self.out_ref.at[where], self.sem)
            copy.start()
            copy.wait()
        recv(self.core, self.far)


def pair_order(i):
    return i + 1 - 2 * (i % 2)


def fused_feed_forward(
    len_ref, cot_ref, a2_ref, a2t_ref, h1_ref, far1_ref, far2_ref, rows_ref,
    out_ref, fold_ref, work_ref, dh1_ref, gb_ref, gbt_ref, sums_ref,
    gf_ref, gft_ref, feed_ref, da2_ref, h_ref, df_ref, weights_ref, turned_ref, missing_ref,
    stage_ref, land_ref, near_ref, cross_ref,
    send_sem, recv_sem, local_sem,
):
    t = pl.program_id(0)
    n = gf_ref.shape[0]
    step = 256
    depth = stage_ref.shape[-2]
    place = Place()
    length = len_ref[place.t]
    links = Links(send_sem, recv_sem)
    y, other = place.y, place.other_y
    last = [
        links.add(place.to_x, far1_ref.at[0, :, other], missing_ref.at[0, 0]),
        links.add(place.to_y, far2_ref.at[2, :, y], missing_ref.at[1, 0]),
    ]
    last_core = [
        links.add(place.to_core, missing_ref.at[i, 0], missing_ref.at[i, 1]) for i in range(2)
    ]
    core = [
        [links.add(place.to_core, stage_ref.at[i], land_ref.at[s, i]) for i in range(2)]
        for s in range(2)
    ]
    cross = [
        links.add(place.to_y, near_ref.at[i, :, other], cross_ref.at[i]) for i in range(2)
    ]
    fetch = pltpu.make_async_copy(cot_ref.at[place.t], gf_ref, local_sem.at[0])
    k = pair_order(t)
    mine = place.group(k)

    def load(step, whole, slot):
        for i, far_ref in enumerate([far1_ref, far2_ref]):
            group = far_ref.at[pair_order(step)]
            to = weights_ref.at[slot, i]
            if not whole:
                group, to = group.at[:, y], to.at[:, y]
            yield pltpu.make_async_copy(group, to, local_sem.at[1 + 2 * slot + i])

    def live_rows(b):
        at = b * step + lax.broadcasted_iota(jnp.int32, (step, 1), 0)
        return (at < length).astype(F32)

    @pl.when(t == 0)
    def _():
        fetch.start()
        for copy in load(0, True, 0):
            copy.start()
        place.greet()
        start(last)
        sums_ref[...] = jnp.zeros_like(sums_ref)
        feed_ref[...] = jnp.zeros_like(feed_ref)
        da2_ref[...] = jnp.zeros_like(da2_ref)
        fetch.wait()

        @pl.loop(0, n // step)
        def _(b):
            rows = pl.ds(pl.multiple_of(b * step, step), step)
            g = (gf_ref[rows, :].astype(F32) * live_rows(b)).astype(BF16)
            gf_ref[rows, :] = g
            gft_ref[:, rows] = g.T
            sums_ref[7:8, :] += jnp.sum(g.astype(F32), 0, keepdims=True)

    for i in range(4):
        @pl.when(t == i)
        def _():
            if i == 2:
                recv(last_core)
            for copy in load(i, i < 2, i % 2):
                copy.wait()
            if i < 3:
                for copy in load(i + 1, i + 1 < 2, (i + 1) % 2):
                    copy.start()
            if i >= 2:
                for j in range(2):
                    weights_ref[i % 2, j, :, other] = missing_ref[j, 3 - i]

    for i in range(2):
        turned_ref[i] = weights_ref[t % 2, i].reshape(D, -1).T

    bias = rows_ref[pl.ds(8 + mine, 1), :]
    w1 = weights_ref[t % 2, 0].reshape(D, -1)
    w2 = weights_ref[t % 2, 1].reshape(D, -1)
    column = jnp.zeros((1, w1.shape[1]), F32)
    for rows in blocks(n, step):
        f = dot_nn(a2_ref[rows, :], w1) + bias
        dh = dot_nn(gf_ref[rows, :], w2)
        f2 = f * f
        th = jnp.tanh(f * (SQRT_2_PI + (SQRT_2_PI * 0.044715) * f2))
        half = 0.5 + 0.5 * th
        h = (f * half).astype(BF16)
        slope = half + f * (0.5 - 0.5 * th * th) * (
            SQRT_2_PI + (3 * SQRT_2_PI * 0.044715) * f2
        )
        df = (dh * slope).astype(BF16)
        h_ref[rows, :] = h
        df_ref[rows, :] = df
        column += jnp.sum(df.astype(F32), 0, keepdims=True)
        feed_ref[rows, :] += dot_nn(h, turned_ref[1])
        da2_ref[rows, :] += dot_nn(df, turned_ref[0])
    sums_ref[pl.ds(8 + mine, 1), :] = column

    @pl.when(t == 1)
    def _():
        recv(last)
        start(last_core)

    def weight_grad(left_ref, right_ref):
        value = dot_nn(left_ref[...], right_ref[...])
        return value.reshape(Z_DEV, Y_DEV, depth, value.shape[-1]).astype(BF16)

    grad1 = weight_grad(a2t_ref, df_ref)
    grad2 = weight_grad(gft_ref, h_ref)

    def put(ref):
        ref[0] = grad1
        ref[1] = grad2

    def reduced(ref):
        return lambda i, s, z: (
            ref[i, z].astype(F32) + land_ref[s, i, z].astype(F32)
        ).astype(BF16)

    @pl.when(t == 0)
    def _():
        put(stage_ref)
        start(core[0])

    @pl.when(t == 1)
    def _():
        put(near_ref)
        recv(core[0])

        @pl.loop(0, Z_DEV)
        def _(z):
            for i in range(2):
                near_ref[i, z] = reduced(near_ref)(i, 0, z)

        start(cross)

    @pl.when(t == 2)
    def _():
        for copy in core[0]:
            copy.wait_send()
        put(stage_ref)
        start(core[1])

    @pl.when(t == 3)
    def _():
        put(work_ref)

        @pl.loop(0, n // step)
        def _(b):
            rows = pl.ds(pl.multiple_of(b * step, step), step)
            live = live_rows(b)
            h1 = h1_ref[rows, :]
            out_ref[rows, :] = (live * (h1 + (feed_ref[rows, :] + rows_ref[7:8, :]))).astype(BF16)
            xhat, r = norm_parts(h1)
            da2 = da2_ref[rows, :]
            sums_ref[1:2, :] += jnp.sum(da2 * xhat, 0, keepdims=True)
            sums_ref[6:7, :] += jnp.sum(da2, 0, keepdims=True)
            dg = da2 * rows_ref[1:2, :]
            dv = r * (
                dg
                - jnp.mean(dg, -1, keepdims=True)
                - xhat * jnp.mean(dg * xhat, -1, keepdims=True)
            )
            dh1 = gf_ref[rows, :].astype(F32) + dv
            dh1_ref[rows, :] = dh1
            gb = dh1.astype(BF16)
            gb_ref[rows, :] = gb
            gbt_ref[:, rows] = gb.T
            sums_ref[5:6, :] += jnp.sum(gb.astype(F32), 0, keepdims=True)

        recv(core[1])

        @pl.loop(0, Z_DEV)
        def _(z):
            for i in range(2):
                work_ref[i, z] = reduced(work_ref)(i, 1, z)

        recv(cross)

        @pl.loop(0, Z_DEV)
        def _(z):
            for i in range(2):
                fold_ref[i, z] = (
                    near_ref[i, z, y].astype(F32) + cross_ref[i, z].astype(F32)
                ).astype(BF16)

        links.sent(*core[0])


def run_fused_feed_forward(lengths, cot, a2, a2t, h1, g1, g2, rows):
    n = cot.shape[1]
    groups, _, _, depth, hidden = g1.shape
    both = (2, Z_DEV, Y_DEV, depth, hidden)
    fold = (2, Z_DEV, depth, hidden)
    return pl.pallas_call(
        fused_feed_forward,
        grid=(groups,),
        in_specs=[SMEM_WHOLE, ANY_WHOLE] + [VMEM_WHOLE] * 3 + [ANY_WHOLE] * 2
        + [VMEM_WHOLE],
        out_specs=[VMEM_WHOLE] * 7,
        out_shape=[
            shaped(BF16, n, D), shaped(BF16, *fold), shaped(BF16, *both), shaped(F32, n, D),
            shaped(BF16, n, D), shaped(BF16, D, n), shaped(F32, 16, D),
        ],
        scratch_shapes=[
            pltpu.VMEM((n, D), BF16), pltpu.VMEM((D, n), BF16), pltpu.VMEM((n, D), F32),
            pltpu.VMEM((n, D), F32), pltpu.VMEM((n, hidden), BF16), pltpu.VMEM((n, hidden), BF16),
            pltpu.VMEM((2,) + both, BF16), pltpu.VMEM((2, hidden, D), BF16),
            pltpu.VMEM((2,) + fold, BF16), pltpu.VMEM(both, BF16), pltpu.VMEM((2,) + both, BF16),
            pltpu.VMEM(both, BF16), pltpu.VMEM(fold, BF16),
            pltpu.SemaphoreType.DMA((10,)), pltpu.SemaphoreType.DMA((10,)),
            pltpu.SemaphoreType.DMA((5,)),
        ],
        compiler_params=pltpu.CompilerParams(
            vmem_limit_bytes=VMEM_LIMIT, collective_id=1, has_side_effects=True
        ),
        name="fused_feed_forward",
    )(lengths, cot, a2, a2t, h1, g1, g2, rows)
class Reduce:
    def __init__(
        self, links, place, work, acc, cross_ref, far_ref, mid_ref, last_ref, side_ref,
        slots=(0, 1),
    ):
        self.place, self.work, self.acc = place, work, acc
        self.cross_ref, self.far_ref, self.mid_ref = cross_ref, far_ref, mid_ref
        self.last_ref, self.side_ref = last_ref, side_ref
        zs = place.zs
        self.y = {
            s: [
                links.add(place.to_y, work(s, zs[j], place.other_y), cross_ref.at[s, zs[j]])
                for j in (1, 3, 2, 0)
            ]
            for s in slots
        }
        self.z = [
            [
                links.add(place.to_z[1], acc(s, zs[1]), far_ref.at[s, 0]),
                links.add(place.to_z[1], acc(s, zs[3]), far_ref.at[s, 1]),
                links.add(place.to_z[2], mid_ref.at[s, 1], far_ref.at[s, 2]),
            ]
            for s in range(2)
        ]
        self.x = links.add(place.to_x, last_ref, side_ref)

    def fold_y(self, s):
        for i, j in enumerate((1, 3, 2, 0)):
            z = self.place.zs[j]
            recv(self.y[s][i])
            value = self.work(s, z, self.place.y)[...].astype(F32)
            self.acc(s, z)[...] = (value + self.cross_ref[s, z].astype(F32)).astype(BF16)
            if i < 2:
                start(self.z[s][i])

    def fold_z(self, s):
        recv(self.z[s][:2])
        for i in (1, 0):
            value = self.acc(s, self.place.zs[2 * i])[...].astype(F32)
            self.mid_ref[s, i] = (value + self.far_ref[s, i].astype(F32)).astype(BF16)
            if i:
                start(self.z[s][2])

    def own(self, s):
        recv(self.z[s][2])
        return self.mid_ref[s, 0].astype(F32) + self.far_ref[s, 2].astype(F32)

    def send_x(self):
        self.last_ref[...] = self.own(1).astype(BF16)
        start(self.x)

    def total(self):
        value = self.own(0)
        recv(self.x)
        return value + self.side_ref[...].astype(F32)


def fused_backward(
    tokens_ref, gqt_ref, gw_ref, rows_ref, dh1_ref, gb_ref, gbt_ref, q_ref, v_ref, kt_ref,
    p_ref, scale_ref, o_ref, ot_ref, a1t_ref, layer_ref, fold_ref, work_ref, early_ref,
    out_ref, layerout_ref, part0_ref, partw_ref, part1_ref, part2_ref, total_ref,
    do_ref, dot_ref, delta_ref, dqt_ref, dqkv_ref, da1_ref, own_ref, passing_ref, passlayer_ref, bqv_ref,
    folded_ref, cross1_ref, far1_ref, mid1_ref, last1_ref, side1_ref,
    cross2_ref, far2_ref, mid2_ref, last2_ref, side2_ref,
    stagew_ref, landw_ref, workw_ref, crossw_ref, farw_ref, midw_ref, lastw_ref, sidew_ref,
    stage0_ref, land0_ref, work0_ref, cross0_ref, far0_ref, mid0_ref, last0_ref, side0_ref,
    sums_ref, sumland_ref,
    send_sem, recv_sem, local_sem,
):
    t = pl.program_id(0)
    n = own_ref.shape[0]
    width = gw_ref.shape[-1]
    depth = part0_ref.shape[0]
    heads = width // HEAD_DIM
    step = n // 4
    place = Place()
    y = place.y
    links = Links(send_sem, recv_sem)
    k, b = group_and_block(t)
    mine = place.group(k)
    now = k % 2
    out = Result(links, place, own_ref, passing_ref, out_ref, step, local_sem.at[0])
    layer = Result(links, place, layer_ref, passlayer_ref, layerout_ref, step, local_sem.at[1])
    fetch = pltpu.make_async_copy(tokens_ref.at[place.t], own_ref, local_sem.at[2])
    corew = [links.add(place.to_core, stagew_ref.at[i], landw_ref.at[i]) for i in range(2)]
    core0 = [links.add(place.to_core, stage0_ref.at[i], land0_ref.at[i]) for i in range(2)]
    def half_done(i, *landing):
        return Reduce(
            links, place, lambda s, z, y: work_ref.at[i, z, y],
            lambda s, z: folded_ref.at[i, z] if s else fold_ref.at[i, z],
            *landing, slots=(1,),
        )

    seg1 = half_done(0, cross1_ref, far1_ref, mid1_ref, last1_ref, side1_ref)
    seg2 = half_done(1, cross2_ref, far2_ref, mid2_ref, last2_ref, side2_ref)
    segw = Reduce(
        links, place, lambda s, z, y: workw_ref.at[s, z, y],
        lambda s, z: workw_ref.at[s, z, y],
        crossw_ref, farw_ref, midw_ref, lastw_ref, sidew_ref,
    )
    seg0 = Reduce(
        links, place, lambda s, z, y: work0_ref.at[s, z, y],
        lambda s, z: work0_ref.at[s, z, y],
        cross0_ref, far0_ref, mid0_ref, last0_ref, side0_ref,
    )
    sum_core, sum_y, *sum_z, sum_x = [
        links.add(to, sums_ref.at[i], sumland_ref.at[j])
        for j, (i, to) in enumerate(
            zip([0, 1, 2, 2, 2, 3], [place.to_core, place.to_y] + place.to_z[1:] + [place.to_x])
        )
    ]

    def when(point):
        return pl.when(t == point)

    @when(0)
    def _():
        fetch.start()
        place.greet()
        for i in range(4):
            layer.send(i)
        start(seg1.y[1], seg2.y[1])
        start(seg1.z[0][:2], seg2.z[0][:2])
        bqv_ref[...] = jnp.zeros_like(bqv_ref)
        sums_ref[0] = early_ref[...]
        da1_ref[...] = jnp.zeros_like(da1_ref)
        fetch.wait()

    for i, point in enumerate([4, 6, 9, 11]):
        @when(point)
        def _():
            layer.pass_on(i)

    @when(4)
    def _():
        seg1.fold_z(0)
        seg2.fold_z(0)

    @when(5)
    def _():
        seg1.fold_y(1)

    @when(8)
    def _():
        seg1.fold_z(1)

    @when(9)
    def _():
        seg2.fold_y(1)

    @when(10)
    def _():
        segw.fold_y(0)
        seg1.send_x()

    @when(11)
    def _():
        recv(corew[1])

        @pl.loop(0, Z_DEV)
        def _(z):
            workw_ref[1, z] = (
                workw_ref[1, z].astype(F32) + landw_ref[1, z].astype(F32)
            ).astype(BF16)

        start(segw.y[1])

    @when(12)
    def _():
        seg2.fold_z(1)
        segw.fold_z(0)

    @when(13)
    def _():
        seg0.fold_y(0)

    @when(14)
    def _():
        segw.fold_y(1)
        seg2.send_x()

    @when(15)
    def _():
        seg0.fold_z(0)
        segw.fold_z(1)

    @pl.when((t == 0) | (t == 4) | (t == 8) | (t == 9))
    def _():
        @pl.loop(0, n // step)
        def _(i):
            rows = pl.ds(pl.multiple_of(i * step, step), step)
            columns = scale_ref[0, :, rows].T
            lane = lax.broadcasted_iota(jnp.int32, (step, width), 1)
            scale = columns[:, heads - 1 : heads]
            for h in reversed(range(heads - 1)):
                scale = jnp.where(lane < (h + 1) * HEAD_DIM, columns[:, h : h + 1], scale)
            do = (dot_nn(gb_ref[rows, :], gw_ref[0]) * scale).astype(BF16)
            do_ref[now, rows, :] = do
            dot = do.T
            dot_ref[now, :, rows] = dot
            product = dot.astype(F32) * ot_ref[0, :, rows].astype(F32)
            for h in range(heads):
                head = slice(h * HEAD_DIM, (h + 1) * HEAD_DIM)
                delta_ref[now, h : h + 1, rows] = jnp.sum(product[head], 0, keepdims=True)

        dqt_ref[now] = jnp.zeros(dqt_ref.shape[1:], F32)
        value = dot_nn(gbt_ref[...], o_ref[0]).reshape(Z_DEV, Y_DEV, depth, width)
        for i in range(2):
            @when(8 * i)
            def _():
                stagew_ref[i] = value.astype(BF16)
                start(corew[i])

        @when(4)
        def _():
            recv(corew[0])
            workw_ref[0] = (value + landw_ref[0].astype(F32)).astype(BF16)
            start(segw.y[0])

        @when(9)
        def _():
            workw_ref[1] = value.astype(BF16)

    for bb in range(4):
        @pl.when(b == bb)
        def _():
            first, last = bb * step, (bb + 1) * step
            do = do_ref[now, first:, :]
            dot = dot_ref[now, :, first:]
            q = q_ref[0, first:, :]
            v = v_ref[0, first:last, :]
            lane = lax.broadcasted_iota(jnp.int32, (1, width), 1)
            dk, dv = None, None
            for h in range(heads):
                lanes = head_mask((1, width), h)
                zero = jnp.zeros((), BF16)
                p = p_ref[0, h, :, first:]
                dp = dot_nn(jnp.where(lanes, v, zero), dot)
                ds = (p.astype(F32) * (dp - delta_ref[now, h : h + 1, first:])).astype(BF16)
                part = dot_nn(p, do)
                dv = part if dv is None else jnp.where(lane < h * HEAD_DIM, dv, part)
                part = dot_nn(ds, q)
                dk = part if dk is None else jnp.where(lane < h * HEAD_DIM, dk, part)
                head = slice(h * HEAD_DIM, (h + 1) * HEAD_DIM)
                dqt_ref[now, head, first:] += dot_nn(kt_ref[0, head, first:last], ds)
            dk = dk.astype(BF16)
            dv = dv.astype(BF16)
            dq = (dqt_ref[now, :, first:last] * HEAD_DIM ** -0.5).astype(BF16).T
            dqkv_ref[now, first:last, :width] = dq
            dqkv_ref[now, first:last, width : 2 * width] = dk
            dqkv_ref[now, first:last, 2 * width :] = dv
            bqv_ref[mine, 0:1, :] += jnp.sum(dq.astype(F32), 0, keepdims=True)
            bqv_ref[mine, 1:2, :] += jnp.sum(dv.astype(F32), 0, keepdims=True)
            da1_ref[first:last, :] += dot_nn(dqkv_ref[now, first:last, :], gqt_ref[0])

    @pl.when((t > 8) & (t % 2 == 1))
    def _():
        rows = pl.ds(pl.multiple_of(b * step, step), step)
        xhat, r = norm_parts(own_ref[rows, :].astype(F32))
        da1 = da1_ref[rows, :]
        sums_ref[0, 0:1, :] += jnp.sum(da1 * xhat, 0, keepdims=True)
        sums_ref[0, 2:3, :] += jnp.sum(da1, 0, keepdims=True)
        dg = da1 * rows_ref[0:1, :]
        dv = r * (
            dg
            - jnp.mean(dg, -1, keepdims=True)
            - xhat * jnp.mean(dg * xhat, -1, keepdims=True)
        )
        own_ref[rows, :] = (dh1_ref[rows, :] + dv).astype(BF16)
        for i in range(4):
            @pl.when(b == i)
            def _():
                out.send(i)

    @pl.when((t == 3) | (t == 7) | (t > 13))
    def _():
        value = dot_nn(a1t_ref[...], dqkv_ref[now]).reshape(Z_DEV, Y_DEV, depth, 3 * width)
        for i in range(2):
            @when(3 + 11 * i)
            def _():
                stage0_ref[i] = value.astype(BF16)
                start(core0[i])

            @when(7 + 8 * i)
            def _():
                recv(core0[i])
                work0_ref[i] = (value + land0_ref[i].astype(F32)).astype(BF16)
                start(seg0.y[i])

    @when(15)
    def _():
        for s in range(4):
            sums_ref[0, 3:5, s * width : (s + 1) * width] = bqv_ref[s, 0:2, :]
        start(sum_core)
        segw.send_x()
        recv(sum_core)
        sums_ref[1] = sums_ref[0] + sumland_ref[0]
        start(sum_y)
        seg0.fold_y(1)
        recv(sum_y)
        sums_ref[2] = sums_ref[1] + sumland_ref[1]
        start(sum_z)
        out.pass_on(0)
        seg0.fold_z(1)
        recv(sum_z)
        sums_ref[3] = (sums_ref[2] + sumland_ref[2]) + (sumland_ref[3] + sumland_ref[4])
        start(sum_x)
        seg0.send_x()
        part1_ref[...] = seg1.total()
        out.pass_on(1)
        layer.finish()
        part2_ref[...] = seg2.total()
        out.pass_on(2)
        partw_ref[...] = segw.total()
        out.pass_on(3)
        recv(sum_x)
        total_ref[...] = sums_ref[3] + sumland_ref[5]
        part0_ref[...] = seg0.total()
        out.finish()
        links.sent()


def group_and_block(t):
    early = t < 8
    return (
        jnp.where(early, 1 - t // 4, 3 - t % 2),
        jnp.where(early, t % 4, jnp.maximum(t - 8, 0) // 2),
    )


def run_fused_backward(
    tokens, gqt, gw, rows, dh1, gb, gbt, q, v, kt, p, scale, o, ot, a1t, layer, fold, work,
    early,
):
    groups, n, _ = tokens.shape
    width = gw.shape[-1]
    heads = width // HEAD_DIM
    hidden = fold.shape[-1]
    depth = D // (Z_DEV * Y_DEV)
    step = n // 4

    def by_group(*shape):
        return pl.BlockSpec(
            (1,) + shape, lambda t: (group_and_block(t)[0],) + (0,) * len(shape)
        )

    p_spec = pl.BlockSpec(
        (1, heads, step, n),
        lambda t: (group_and_block(t)[0], 0, group_and_block(t)[1], 0),
    )

    def early_group(*shape):
        return pl.BlockSpec(
            (1,) + shape, lambda t: (group_and_block(jnp.minimum(t, 9))[0],) + (0,) * len(shape)
        )

    copies = 2 * 12 + 4 + 2 * 15 + 2 * 11 + 6

    def landing(lanes):
        return [
            pltpu.VMEM((2, Z_DEV, depth, lanes), BF16),
            pltpu.VMEM((2, 3, depth, lanes), BF16), pltpu.VMEM((2, 2, depth, lanes), BF16),
            pltpu.VMEM((depth, lanes), BF16), pltpu.VMEM((depth, lanes), BF16),
        ]

    def working(lanes):
        return [pltpu.VMEM((2, Z_DEV, Y_DEV, depth, lanes), BF16)] * 3

    return pl.pallas_call(
        fused_backward,
        grid=(4 * groups,),
        in_specs=[
            ANY_WHOLE, by_group(3 * width, D), early_group(D, width), VMEM_WHOLE, VMEM_WHOLE,
            VMEM_WHOLE, VMEM_WHOLE, by_group(n, width), by_group(n, width),
            by_group(width, n), p_spec, early_group(8, n), early_group(n, width),
            early_group(width, n),
            VMEM_WHOLE, VMEM_WHOLE, VMEM_WHOLE, VMEM_WHOLE, VMEM_WHOLE,
        ],
        out_specs=[ANY_WHOLE] * 2 + [VMEM_WHOLE] * 5,
        out_shape=[
            shaped(BF16, groups, n, D), shaped(BF16, groups, n, D),
            shaped(F32, depth, 3 * width),
            shaped(F32, depth, width), shaped(F32, depth, hidden),
            shaped(F32, depth, hidden), shaped(F32, 16, D),
        ],
        scratch_shapes=[
            pltpu.VMEM((2, n, width), BF16), pltpu.VMEM((2, width, n), BF16),
            pltpu.VMEM((2, 8, n), F32), pltpu.VMEM((2, width, n), F32),
            pltpu.VMEM((2, n, 3 * width), BF16), pltpu.VMEM((n, D), F32),
            pltpu.VMEM((n, D), BF16), pltpu.VMEM((n, D), BF16), pltpu.VMEM((n, D), BF16),
            pltpu.VMEM((groups, 8, width), F32),
        ]
        + landing(hidden)[:1] + landing(hidden) + landing(hidden)
        + working(width) + landing(width)
        + working(3 * width) + landing(3 * width)
        + [
            pltpu.VMEM((4, 16, D), F32), pltpu.VMEM((6, 16, D), F32),
            pltpu.SemaphoreType.DMA((copies,)), pltpu.SemaphoreType.DMA((copies,)),
            pltpu.SemaphoreType.DMA((3,)),
        ],
        compiler_params=pltpu.CompilerParams(
            vmem_limit_bytes=VMEM_LIMIT, collective_id=2, has_side_effects=True
        ),
        name="fused_backward",
    )(
        tokens, gqt, gw, rows, dh1, gb, gbt, q, v, kt, p, scale, o, ot, a1t, layer, fold, work,
        early,
    )


def place_gradients(
    tie_ref, sums_ref, part0_ref, partw_ref, part1_ref, part2_ref, near_out_ref,
    near_grad_ref, far_out_ref, far_grad_ref, gains_ref, bias_ref, in_ref, out_ref, expand_ref,
    project_ref,
):
    far_out_ref[...] = near_out_ref[...]
    far_grad_ref[...] = near_grad_ref[...]
    own = gains_ref.shape[-1]
    width = partw_ref.shape[-1]

    @pl.when(pl.program_id(0) == 0)
    def _():
        first = (lax.axis_index("dp") * 4 + lax.axis_index("tensor")) * own
        feature = lax.broadcasted_iota(jnp.int32, (D, 128), 0)
        lane = lax.broadcasted_iota(jnp.int32, (D, 128), 1)
        chosen = ((feature == first + lane) & (lane < own)).astype(F32)
        sums = lax.dot_general(
            sums_ref[...], chosen, (((1,), (0,)), ((), ())),
            precision=lax.Precision.HIGHEST, preferred_element_type=F32,
        )[:, :own]
        s0, s1, s2, s3 = tie_ref[0], tie_ref[1], tie_ref[2], tie_ref[3]
        w_out = partw_ref[...].T

        def at(source, wanted, value):
            return jnp.where(source == wanted, value, jnp.zeros_like(value))

        row = lax.broadcasted_iota(jnp.int32, (NSRC, own), 0)
        for i, wanted in enumerate([s0, s0, s0, s1, s2, s3, s2, s2, s2, s2]):
            bias_ref[i] = jnp.where(row == wanted, sums[2 + i : 3 + i], 0.0)
        for s in range(NSRC):
            gains_ref[s, 0:1] = at(s, s0, sums[0:1])
            gains_ref[s, 1:2] = at(s, s2, sums[1:2])
            for j in range(3):
                in_ref[s, j] = at(s, s0, part0_ref[:, j * width : (j + 1) * width])
            out_ref[s] = at(s, s1, w_out)
            expand_ref[s] = at(s, s2, part1_ref[...])
            project_ref[s] = at(s, s3, part2_ref[...])


def run_place_gradients(tie, sums, part0, partw, part1, part2, out, grad, like):
    slots, n, _ = grad.shape
    gains, biases, w_in, w_out, w_expand, w_project = [item.shape for item in like]
    shapes = [
        gains, (biases[1], biases[0], biases[2]), w_in, w_out, w_expand,
        (w_project[0], w_project[2], w_project[1]),
    ]
    out, grad, gains, biases, w_in, w_out, w_expand, w_project = pl.pallas_call(
        place_gradients,
        grid=(slots,),
        in_specs=[SMEM_WHOLE] + [VMEM_WHOLE] * 5
        + [group(n, D), group(n, D)],
        out_specs=[group(n, D), group(n, D)] + [VMEM_WHOLE] * 6,
        out_shape=[shaped(BF16, slots, n, D)] * 2 + [shaped(F32, *item) for item in shapes],
        compiler_params=pltpu.CompilerParams(vmem_limit_bytes=VMEM_LIMIT),
        name="place_gradients",
    )(tie, sums, part0, partw, part1, part2, out, grad)
    biases = biases.transpose(1, 0, 2)
    return out, grad, gains, biases, w_in, w_out, w_expand, w_project.transpose(0, 2, 1)


def plain_step(
    tokens, lengths, tie_map, norm_gains, bias_rows, attention_in, attention_out,
    expand_weight, project_weight, cotangent,
):
    slot_rows = tokens.shape[0] // lengths.shape[0]
    me = lax.axis_index("tensor")
    in_local = lax.dynamic_index_in_dim(attention_in, tie_map[0], 0, keepdims=False)
    out_local = lax.dynamic_index_in_dim(attention_out, tie_map[1], 0, keepdims=False)
    expand_local = lax.dynamic_index_in_dim(expand_weight, tie_map[2], 0, keepdims=False)
    project_local = lax.dynamic_index_in_dim(project_weight, tie_map[3], 0, keepdims=False)
    local0 = jnp.concatenate([in_local, out_local.T[None]], 0)
    row_kinds = jnp.array([0, 0, 0, 1, 2, 3] + [2] * (FF // D), dtype=jnp.int32)
    gain_kinds = jnp.array([0, 2], dtype=jnp.int32)
    gain_pick = norm_gains[tie_map[gain_kinds], jnp.arange(2)]
    bias_pick = bias_rows[tie_map[row_kinds], jnp.arange(row_kinds.shape[0])]
    vectors = jnp.concatenate([gain_pick, bias_pick], 0)
    x = lax.dynamic_slice_in_dim(tokens, me * slot_rows, slot_rows, 0)
    cot = lax.dynamic_slice_in_dim(cotangent, me * slot_rows, slot_rows, 0)
    length = lax.dynamic_slice_in_dim(lengths, me, 1, 0)
    rows = lax.all_gather(vectors, ("dp", "tensor"), axis=1, tiled=True).astype(F32)
    rows = jnp.concatenate([rows, jnp.zeros((4, D), F32)], 0)

    def gathered(piece, axis):
        piece = lax.all_gather(piece, "dp", axis=axis, tiled=True)
        return lax.all_gather(piece, "tensor", axis=0)

    g0 = gathered(local0, 1)
    g1 = gathered(expand_local, 0)
    g2 = gathered(project_local.T, 0)
    groups, width = g0.shape[0], g0.shape[-1]
    bqv = rows[3:5].reshape(2, groups, width).transpose(1, 0, 2)
    q, v, kt, p, o, a1t, h1, a2, a2t = run_attention_forward(length, x, g0, rows, bqv)
    out, d1, d2, dh1, gb, gbt, sums = run_feed_forward(length, cot, a2, a2t, h1, g1, g2, rows)
    d0, xg, sums_in, sums_qv = run_attention_backward(
        x, g0, rows, dh1, gb, gbt, q, v, kt, p, o, a1t
    )
    layer_out = lax.all_gather(out, "tensor", axis=0, tiled=True)
    tokens_grad = lax.all_gather(xg, "tensor", axis=0, tiled=True)

    def scattered(piece, axis):
        piece = lax.psum_scatter(piece, "tensor", scatter_dimension=0)
        return lax.psum_scatter(piece, "dp", scatter_dimension=axis, tiled=True).astype(F32)

    part0 = scattered(d0, 1)
    part1 = scattered(d1, 0)
    part2 = scattered(d2, 0)
    qv = sums_qv[:, :2].transpose(1, 0, 2).reshape(2, D)
    sums = jnp.concatenate(
        [sums_in[0:1], sums[1:2], sums_in[1:2], qv, sums[5:12]], 0
    )
    sums = lax.psum_scatter(sums, ("dp", "tensor"), scatter_dimension=1, tiled=True)
    return layer_out, tokens_grad, *placed(tie_map, sums, part0, part1, part2)


def fused_step(
    tokens, lengths, tie_map, norm_gains, bias_rows, attention_in, attention_out,
    expand_weight, project_weight, cotangent,
):
    slots = lengths.shape[0]
    tokens = tokens.reshape(slots, -1, D)
    cotangent = cotangent.reshape(slots, -1, D)
    gqt, gw, g1, g2, rows, q, v, kt, p, scale, o, ot, a1t, h1, a2, a2t = run_fused_forward(
        tie_map, lengths, tokens, norm_gains, bias_rows, attention_in, attention_out,
        expand_weight, project_weight,
    )
    layer, fold, work, dh1, gb, gbt, early = run_fused_feed_forward(
        lengths, cotangent, a2, a2t, h1, g1, g2, rows
    )
    grad, out, part0, partw, part1, part2, sums = run_fused_backward(
        tokens, gqt, gw, rows, dh1, gb, gbt, q, v, kt, p, scale, o, ot, a1t, layer, fold,
        work, early,
    )
    out, grad, *placed_grads = run_place_gradients(
        tie_map, sums, part0, partw, part1, part2, out, grad,
        (norm_gains, bias_rows, attention_in, attention_out, expand_weight, project_weight),
    )
    return out.reshape(-1, D), grad.reshape(-1, D), *placed_grads


def placed(tie_map, sums, part0, part1, part2):
    source = jnp.arange(NSRC, dtype=jnp.int32)

    def place(piece, which):
        pick = (source == tie_map[which]).reshape((NSRC,) + (1,) * piece.ndim)
        return jnp.where(pick, piece[None], 0.0)

    def place_rows(piece, kinds):
        pick = source[:, None] == tie_map[jnp.array(kinds, dtype=jnp.int32)][None, :]
        return jnp.where(pick[:, :, None], piece[None], 0.0)

    return (
        place_rows(sums[:2], [0, 2]),
        place_rows(sums[2:], [0, 0, 0, 1, 2, 3] + [2] * (FF // D)),
        place(part0[:3], 0),
        place(part0[3].T, 1),
        place(part1, 2),
        place(part2.T, 3),
    )


def solution(mesh):
    fused = mesh.shape["dp"] == Z_DEV * Y_DEV and mesh.shape["tensor"] == X_DEV * C_DEV
    return jax.shard_map(
        fused_step if fused else plain_step,
        mesh=mesh,
        in_specs=(
            P("dp", None),
            P("dp"),
            P(),
            P(None, None, ("dp", "tensor")),
            P(None, None, ("dp", "tensor")),
            P(None, None, "dp", "tensor"),
            P(None, "tensor", "dp"),
            P(None, "dp", "tensor"),
            P(None, "tensor", "dp"),
            P("dp", None),
        ),
        out_specs=(
            P("dp", None),
            P("dp", None),
            P(None, None, ("dp", "tensor")),
            P(None, None, ("dp", "tensor")),
            P(None, None, "dp", "tensor"),
            P(None, "tensor", "dp"),
            P(None, "dp", "tensor"),
            P(None, "tensor", "dp"),
        ),
        check_vma=False,
    )
```

```python
import jax
import jax.numpy as jnp
from jax import lax
from jax.experimental import pallas as pl
from jax.experimental.pallas import tpu as pltpu
from jax.sharding import PartitionSpec as P

D = 768
HEAD_DIM = 64
FF = 3072
NSRC = 4
EPS = 1e-05
MASKED = -1e30
F32 = jnp.float32
BF16 = jnp.bfloat16
VMEM_LIMIT = 60 * 1024 * 1024


def dot_nn(a, b):
    return lax.dot_general(a, b, (((1,), (0,)), ((), ())), preferred_element_type=F32)


def dot_nt(a, b):
    return lax.dot_general(a, b, (((1,), (1,)), ((), ())), preferred_element_type=F32)


def norm_parts(v):
    center = jnp.mean(v, -1, keepdims=True)
    centered = v - center
    r = lax.rsqrt(jnp.mean(centered * centered, -1, keepdims=True) + EPS)
    return centered * r, r


def head_mask(shape, h):
    lane = lax.broadcasted_iota(jnp.int32, shape, 1)
    return (lane >= h * HEAD_DIM) & (lane < (h + 1) * HEAD_DIM)


def blocks(total, size):
    return [slice(i * size, (i + 1) * size) for i in range(total // size)]


def attention_forward(
    len_ref, x_ref, g_ref, rows_ref, bqv_ref,
    q_ref, v_ref, kt_ref, p_ref, o_ref, a1t_ref, h1_ref, a2_ref, a2t_ref,
    a1_ref, k_ref, vt_ref, ot_ref, attn_ref,
):
    t = pl.program_id(0)
    n = x_ref.shape[0]
    width = g_ref.shape[-1]
    heads = width // HEAD_DIM
    step = 256
    length = len_ref[0]

    @pl.when(t == 0)
    def _():
        @pl.loop(0, n // step)
        def _(b):
            rows = pl.ds(pl.multiple_of(b * step, step), step)
            xhat, _ = norm_parts(x_ref[rows, :].astype(F32))
            a1 = xhat * rows_ref[0:1, :] + rows_ref[2:3, :]
            a1_ref[rows, :] = a1.astype(BF16)
            a1t_ref[:, rows] = a1.astype(BF16).T
            attn_ref[rows, :] = x_ref[rows, :].astype(F32) + rows_ref[5:6, :]

    @pl.loop(0, n // step)
    def _(b):
        rows = pl.ds(pl.multiple_of(b * step, step), step)
        a1 = a1_ref[rows, :]
        q = (dot_nn(a1, g_ref[0, 0]) + bqv_ref[0, 0:1, :]).astype(BF16)
        q_ref[0, rows, :] = q * jnp.asarray(HEAD_DIM ** -0.5, BF16)
        k = dot_nn(a1, g_ref[0, 1]).astype(BF16)
        k_ref[rows, :] = k
        kt_ref[0, :, rows] = k.T
        v = (dot_nn(a1, g_ref[0, 2]) + bqv_ref[0, 1:2, :]).astype(BF16)
        v_ref[0, rows, :] = v
        vt_ref[:, rows] = v.T

    for h in range(heads):
        k = k_ref[...]
        k = jnp.where(head_mask(k.shape, h), k, jnp.zeros_like(k))
        for b in range(n // step):
            first, last = b * step, (b + 1) * step
            q = q_ref[0, first:last, :]
            key = lax.broadcasted_iota(jnp.int32, (last, step), 0)
            query = lax.broadcasted_iota(jnp.int32, (step, step), 1) + first
            s = dot_nt(k[:last], q)
            near = jnp.where(
                (key[first:] <= query) & (key[first:] < length), s[first:], MASKED
            )
            if b:
                far = jnp.where(key[:first] < length, s[:first], MASKED)
                top = jnp.maximum(
                    jnp.max(far, 0, keepdims=True), jnp.max(near, 0, keepdims=True)
                )
                e_far = jnp.exp(far - top)
                e_near = jnp.exp(near - top)
                total = jnp.sum(e_far, 0, keepdims=True) + jnp.sum(e_near, 0, keepdims=True)
                scale = 1.0 / total
                p_ref[0, h, :first, first:last] = (e_far * scale).astype(BF16)
            else:
                top = jnp.max(near, 0, keepdims=True)
                e_near = jnp.exp(near - top)
                scale = 1.0 / jnp.sum(e_near, 0, keepdims=True)
            p_ref[0, h, first:last, first:last] = (e_near * scale).astype(BF16)
            ot_ref[h * HEAD_DIM : (h + 1) * HEAD_DIM, first:last] = dot_nn(
                vt_ref[h * HEAD_DIM : (h + 1) * HEAD_DIM, :last],
                p_ref[0, h, :last, first:last],
            ).astype(BF16)

    @pl.loop(0, n // step)
    def _(b):
        rows = pl.ds(pl.multiple_of(b * step, step), step)
        o = ot_ref[:, rows].T
        o_ref[0, rows, :] = o
        attn_ref[rows, :] += dot_nt(o, g_ref[0, 3])

    @pl.when(t == pl.num_programs(0) - 1)
    def _():
        @pl.loop(0, n // step)
        def _(b):
            rows = pl.ds(pl.multiple_of(b * step, step), step)
            h1 = attn_ref[rows, :]
            h1_ref[rows, :] = h1
            xhat, _ = norm_parts(h1)
            a2 = (xhat * rows_ref[1:2, :] + rows_ref[6:7, :]).astype(BF16)
            a2_ref[rows, :] = a2
            a2t_ref[:, rows] = a2.T


SQRT_2_PI = 0.7978845608028654


def feed_forward_both(
    len_ref, c_ref, a2_ref, a2t_ref, h1_ref, w1_ref, w2_ref, rows_ref,
    out_ref, d1_ref, d2_ref, dh1_ref, gb_ref, gbt_ref, sums_ref,
    gf_ref, gft_ref, feed_ref, da2_ref, h_ref, df_ref,
):
    t = pl.program_id(0)
    n = c_ref.shape[0]
    step = 256
    length = len_ref[0]

    @pl.when(t == 0)
    def _():
        sums_ref[...] = jnp.zeros_like(sums_ref)

        @pl.loop(0, n // step)
        def _(b):
            rows = pl.ds(pl.multiple_of(b * step, step), step)
            place = b * step + lax.broadcasted_iota(jnp.int32, (step, 1), 0)
            live = (place < length).astype(F32)
            g = (c_ref[rows, :].astype(F32) * live).astype(BF16)
            gf_ref[rows, :] = g
            gft_ref[:, rows] = g.T
            sums_ref[7:8, :] += jnp.sum(g.astype(F32), 0, keepdims=True)

    bias = rows_ref[pl.ds(8 + t, 1), :]

    @pl.loop(0, n // step)
    def _(b):
        rows = pl.ds(pl.multiple_of(b * step, step), step)
        f = dot_nn(a2_ref[rows, :], w1_ref[0]) + bias
        dh = dot_nn(gf_ref[rows, :], w2_ref[0])
        f2 = f * f
        th = jnp.tanh(f * (SQRT_2_PI + (SQRT_2_PI * 0.044715) * f2))
        half = 0.5 + 0.5 * th
        h = (f * half).astype(BF16)
        slope = half + f * (0.5 - 0.5 * th * th) * (
            SQRT_2_PI + (3 * SQRT_2_PI * 0.044715) * f2
        )
        df = (dh * slope).astype(BF16)
        h_ref[rows, :] = h
        df_ref[rows, :] = df
        sums_ref[pl.ds(8 + t, 1), :] += jnp.sum(df.astype(F32), 0, keepdims=True)
        feed = dot_nt(h, w2_ref[0])
        da2 = dot_nt(df, w1_ref[0])

        @pl.when(t == 0)
        def _():
            feed_ref[rows, :] = feed
            da2_ref[rows, :] = da2

        @pl.when(t > 0)
        def _():
            feed_ref[rows, :] += feed
            da2_ref[rows, :] += da2

    @pl.loop(0, D // step)
    def _(b):
        rows = pl.ds(pl.multiple_of(b * step, step), step)
        d1_ref[0, rows, :] = dot_nn(a2t_ref[rows, :], df_ref[...]).astype(BF16)
        d2_ref[0, rows, :] = dot_nn(gft_ref[rows, :], h_ref[...]).astype(BF16)

    @pl.when(t == pl.num_programs(0) - 1)
    def _():
        @pl.loop(0, n // step)
        def _(b):
            rows = pl.ds(pl.multiple_of(b * step, step), step)
            place = b * step + lax.broadcasted_iota(jnp.int32, (step, 1), 0)
            live = (place < length).astype(F32)
            h1 = h1_ref[rows, :]
            out_ref[rows, :] = (live * (h1 + (feed_ref[rows, :] + rows_ref[7:8, :]))).astype(BF16)
            xhat, r = norm_parts(h1)
            da2 = da2_ref[rows, :]
            sums_ref[1:2, :] += jnp.sum(da2 * xhat, 0, keepdims=True)
            sums_ref[6:7, :] += jnp.sum(da2, 0, keepdims=True)
            dg = da2 * rows_ref[1:2, :]
            dv = r * (
                dg
                - jnp.mean(dg, -1, keepdims=True)
                - xhat * jnp.mean(dg * xhat, -1, keepdims=True)
            )
            dh1 = live * c_ref[rows, :].astype(F32) + dv
            dh1_ref[rows, :] = dh1
            gb = dh1.astype(BF16)
            gb_ref[rows, :] = gb
            gbt_ref[:, rows] = gb.T
            sums_ref[5:6, :] += jnp.sum(gb.astype(F32), 0, keepdims=True)


def attention_backward(
    x_ref, g_ref, rows_ref, dh1_ref, gb_ref, gbt_ref, q_ref, v_ref, kt_ref, p_ref,
    o_ref, a1t_ref,
    d0_ref, xg_ref, sums_ref, bqv_ref,
    do_ref, delta_ref, dqt_ref, dq_ref, dk_ref, dv_ref, da1_ref,
):
    t = pl.program_id(0)
    n = x_ref.shape[0]
    width = g_ref.shape[-1]
    heads = width // HEAD_DIM
    step = 256
    pick = (
        lax.broadcasted_iota(jnp.int32, (16, width), 1) // HEAD_DIM
        == lax.broadcasted_iota(jnp.int32, (16, width), 0)
    ).astype(BF16)

    @pl.loop(0, n // step)
    def _(b):
        rows = pl.ds(pl.multiple_of(b * step, step), step)
        do = dot_nn(gb_ref[rows, :], g_ref[0, 3]).astype(BF16)
        do_ref[rows, :] = do
        prod = do.astype(F32) * o_ref[0, rows, :].astype(F32)
        high = prod.astype(BF16)
        low = (prod - high.astype(F32)).astype(BF16)
        delta_ref[:, rows] = dot_nt(pick, high) + dot_nt(pick, low)

    dqt_ref[...] = jnp.zeros_like(dqt_ref)
    for b in range(n // step):
        first, last = b * step, (b + 1) * step
        do = do_ref[first:, :]
        q = q_ref[0, first:, :]
        v = v_ref[0, first:last, :]
        dk, dv = None, None
        for h in range(heads):
            mine = head_mask((1, width), h)
            zero = jnp.zeros((), BF16)
            p = p_ref[0, h, first:last, first:]
            dp = dot_nt(jnp.where(mine, v, zero), do)
            ds = (p.astype(F32) * (dp - delta_ref[h : h + 1, first:])).astype(BF16)
            part = dot_nn(p, jnp.where(mine, do, zero))
            dv = part if dv is None else dv + part
            part = dot_nn(ds, jnp.where(mine, q, zero))
            dk = part if dk is None else dk + part
            head = slice(h * HEAD_DIM, (h + 1) * HEAD_DIM)
            dqt_ref[head, first:] += dot_nn(kt_ref[0, head, first:last], ds)
        dk_ref[first:last, :] = dk.astype(BF16)
        dv_ref[first:last, :] = dv.astype(BF16)

    @pl.when(t == 0)
    def _():
        da1_ref[...] = jnp.zeros_like(da1_ref)

    bqv_ref[...] = jnp.zeros_like(bqv_ref)

    @pl.loop(0, n // step)
    def _(b):
        rows = pl.ds(pl.multiple_of(b * step, step), step)
        dq = (dqt_ref[:, rows] * HEAD_DIM ** -0.5).astype(BF16).T
        dk = dk_ref[rows, :]
        dv = dv_ref[rows, :]
        dq_ref[rows, :] = dq
        bqv_ref[0, 0:1, :] += jnp.sum(dq.astype(F32), 0, keepdims=True)
        bqv_ref[0, 1:2, :] += jnp.sum(dv.astype(F32), 0, keepdims=True)
        da1_ref[rows, :] += (
            dot_nt(dq, g_ref[0, 0]) + dot_nt(dk, g_ref[0, 1]) + dot_nt(dv, g_ref[0, 2])
        )

    @pl.loop(0, D // step)
    def _(b):
        rows = pl.ds(pl.multiple_of(b * step, step), step)
        a1t = a1t_ref[rows, :]
        d0_ref[0, 0, rows, :] = dot_nn(a1t, dq_ref[...]).astype(BF16)
        d0_ref[0, 1, rows, :] = dot_nn(a1t, dk_ref[...]).astype(BF16)
        d0_ref[0, 2, rows, :] = dot_nn(a1t, dv_ref[...]).astype(BF16)
        d0_ref[0, 3, rows, :] = dot_nn(gbt_ref[rows, :], o_ref[0]).astype(BF16)

    @pl.when(t == pl.num_programs(0) - 1)
    def _():
        sums_ref[...] = jnp.zeros_like(sums_ref)

        @pl.loop(0, n // step)
        def _(b):
            rows = pl.ds(pl.multiple_of(b * step, step), step)
            xhat, r = norm_parts(x_ref[rows, :].astype(F32))
            da1 = da1_ref[rows, :]
            sums_ref[0:1, :] += jnp.sum(da1 * xhat, 0, keepdims=True)
            sums_ref[1:2, :] += jnp.sum(da1, 0, keepdims=True)
            dg = da1 * rows_ref[0:1, :]
            dv = r * (
                dg
                - jnp.mean(dg, -1, keepdims=True)
                - xhat * jnp.mean(dg * xhat, -1, keepdims=True)
            )
            xg_ref[rows, :] = (dh1_ref[rows, :] + dv).astype(BF16)


def whole(*shape):
    return pl.BlockSpec(shape, lambda t: (0,) * len(shape))


def group(*shape):
    return pl.BlockSpec((1,) + shape, lambda t: (t,) + (0,) * len(shape))


def shaped(dtype, *shape):
    return jax.ShapeDtypeStruct(shape, dtype)


SMEM_WHOLE = pl.BlockSpec(memory_space=pltpu.SMEM)


def run_attention_forward(length, x, g0, rows, bqv):
    n = x.shape[0]
    groups, _, _, width = g0.shape
    heads = width // HEAD_DIM
    return pl.pallas_call(
        attention_forward,
        grid=(groups,),
        in_specs=[SMEM_WHOLE, whole(n, D), group(4, D, width), whole(16, D), group(2, width)],
        out_specs=[
            group(n, width), group(n, width), group(width, n), group(heads, n, n),
            group(n, width), whole(D, n), whole(n, D), whole(n, D), whole(D, n),
        ],
        out_shape=[
            shaped(BF16, groups, n, width), shaped(BF16, groups, n, width),
            shaped(BF16, groups, width, n), shaped(BF16, groups, heads, n, n),
            shaped(BF16, groups, n, width), shaped(BF16, D, n), shaped(F32, n, D),
            shaped(BF16, n, D), shaped(BF16, D, n),
        ],
        scratch_shapes=[
            pltpu.VMEM((n, D), BF16), pltpu.VMEM((n, width), BF16),
            pltpu.VMEM((width, n), BF16), pltpu.VMEM((width, n), BF16),
            pltpu.VMEM((n, D), F32),
        ],
        compiler_params=pltpu.CompilerParams(vmem_limit_bytes=VMEM_LIMIT),
        name="attention_forward",
    )(length, x, g0, rows, bqv)


def run_feed_forward(length, cot, a2, a2t, h1, g1, g2, rows):
    n = cot.shape[0]
    groups, _, width = g1.shape
    return pl.pallas_call(
        feed_forward_both,
        grid=(groups,),
        in_specs=[
            SMEM_WHOLE, whole(n, D), whole(n, D), whole(D, n), whole(n, D),
            group(D, width), group(D, width), whole(16, D),
        ],
        out_specs=[
            whole(n, D), group(D, width), group(D, width), whole(n, D), whole(n, D),
            whole(D, n), whole(16, D),
        ],
        out_shape=[
            shaped(BF16, n, D), shaped(BF16, groups, D, width), shaped(BF16, groups, D, width),
            shaped(F32, n, D), shaped(BF16, n, D), shaped(BF16, D, n), shaped(F32, 16, D),
        ],
        scratch_shapes=[
            pltpu.VMEM((n, D), BF16), pltpu.VMEM((D, n), BF16), pltpu.VMEM((n, D), F32),
            pltpu.VMEM((n, D), F32), pltpu.VMEM((n, width), BF16), pltpu.VMEM((n, width), BF16),
        ],
        compiler_params=pltpu.CompilerParams(vmem_limit_bytes=VMEM_LIMIT),
        name="feed_forward_both",
    )(length, cot, a2, a2t, h1, g1, g2, rows)


def run_attention_backward(x, g0, rows, dh1, gb, gbt, q, v, kt, p, o, a1t):
    n = x.shape[0]
    groups, _, _, width = g0.shape
    heads = width // HEAD_DIM
    return pl.pallas_call(
        attention_backward,
        grid=(groups,),
        in_specs=[
            whole(n, D), group(4, D, width), whole(16, D), whole(n, D), whole(n, D),
            whole(D, n), group(n, width), group(n, width), group(width, n),
            group(heads, n, n), group(n, width), whole(D, n),
        ],
        out_specs=[group(4, D, width), whole(n, D), whole(8, D), group(8, width)],
        out_shape=[
            shaped(BF16, groups, 4, D, width), shaped(BF16, n, D), shaped(F32, 8, D),
            shaped(F32, groups, 8, width),
        ],
        scratch_shapes=[
            pltpu.VMEM((n, width), BF16), pltpu.VMEM((16, n), F32), pltpu.VMEM((width, n), F32),
            pltpu.VMEM((n, width), BF16), pltpu.VMEM((n, width), BF16),
            pltpu.VMEM((n, width), BF16), pltpu.VMEM((n, D), F32),
        ],
        compiler_params=pltpu.CompilerParams(vmem_limit_bytes=VMEM_LIMIT),
        name="attention_backward",
    )(x, g0, rows, dh1, gb, gbt, q, v, kt, p, o, a1t)


Z_DEV, Y_DEV, X_DEV, C_DEV = 4, 2, 2, 2


class Place:
    def __init__(self):
        dp, self.t = lax.axis_index("dp"), lax.axis_index("tensor")
        self.dp = dp
        self.z, self.y = dp // 2, dp % 2
        self.x, self.c = self.t // 2, self.t % 2
        self.other_y = 1 - self.y
        self.zs = [
            self.z,
            self.z + 1 - 2 * (self.z % 2),
            self.z + 2 - 4 * (self.z // 2),
            3 - self.z,
        ]
        self.ts = [
            self.t,
            self.t + 1 - 2 * (self.t % 2),
            self.t + 2 - 4 * (self.t // 2),
            3 - self.t,
        ]
        self.to_z = [dict(dp=z * 2 + self.y) for z in self.zs]
        self.to_y = dict(dp=self.z * 2 + self.other_y)
        self.to_x = dict(tensor=self.ts[2])
        self.same_t = self.to_z[1:] + [dict(dp=z * 2 + self.other_y) for z in self.zs]
        self.same_dp = [dict(tensor=t) for t in self.ts[1:]]
        self.to_core = dict(tensor=self.ts[1])

    def group(self, k):
        return lax.select(
            k == 0, self.ts[0],
            lax.select(k == 1, self.ts[1], lax.select(k == 2, self.ts[2], self.ts[3])),
        )

    def greet(self, others=None):
        barrier = pltpu.get_barrier_semaphore()
        others = others or self.to_z[1:] + [self.to_y, self.to_x, self.to_core]
        for device in others:
            pl.semaphore_signal(
                barrier, inc=1, device_id=device, device_id_type=pl.DeviceIdType.MESH
            )
        pl.semaphore_wait(barrier, len(others))


class Links:
    def __init__(self, send_sem, recv_sem):
        self.send_sem, self.recv_sem = send_sem, recv_sem
        self.copies = []

    def add(self, device, src, dst):
        number = len(self.copies)
        copy = pltpu.make_async_remote_copy(
            src_ref=src,
            dst_ref=dst,
            send_sem=self.send_sem.at[number],
            recv_sem=self.recv_sem.at[number],
            device_id=device,
            device_id_type=pl.DeviceIdType.MESH,
        )
        self.copies.append(copy)
        return copy

    def sent(self, *apart):
        for copy in self.copies:
            if all(copy is not other for other in apart):
                copy.wait_send()


def flat(copies):
    for item in copies:
        if isinstance(item, list):
            yield from flat(item)
        else:
            yield item


def start(*copies):
    for copy in flat(copies):
        copy.start()


def recv(*copies):
    for copy in flat(copies):
        copy.wait_recv()


class Gather:
    def __init__(self, links, place, own, full, order, single=True, last=True):
        every = slice(None)
        y, other = place.y, place.other_y

        def same(device, k, yy, to):
            return links.add(device, full(k, every, yy), full(to, every, yy))

        def along_z(k, yy, block):
            here, passed = full(k, place.z, yy), full(k, place.zs[2], yy)
            return [
                links.add(place.to_z[1], block, here),
                links.add(place.to_z[2], block, here),
                links.add(place.to_z[1], passed, passed),
            ]

        self.z = along_z(0, y, own)
        if order == X_Z_Y:
            self.first = [links.add(place.to_x, own, full(2, place.z, y))]
            self.far = along_z(2, y, full(2, place.z, y))
            blocks = [(0, y), (2, y), (0, other), (2, other)]
        else:
            blocks = [(0, y), (0, other), (2, y), (2, other)]
        if order == Y_Z_X:
            self.first = [links.add(place.to_y, own, full(0, place.z, y))]
            self.far = along_z(0, other, full(0, place.z, other))
        if order == Z_Y_X and single:
            self.first = [same(place.to_y, 0, y, 0)]
        if order == Z_Y_X and not single:
            self.first = [links.add(place.to_y, own, full(0, place.z, y))]
            for k in range(1, 4):
                block = full(0, place.zs[k], y)
                self.first.append(links.add(place.to_y, block, block))
        if not last:
            blocks = blocks[:-1]
        self.second = [
            same(place.to_y, k, yy, k) if order == X_Z_Y else same(place.to_x, k, yy, 2)
            for k, yy in blocks[:2][: 2 if last else 1]
        ]
        self.core = [same(place.to_core, k, yy, k + 1) for k, yy in blocks]


Z_Y_X, Y_Z_X, X_Z_Y = range(3)


def fused_forward(
    tie_ref, len_ref, tokens_ref, gains_ref, bias_ref, in_ref, out_ref, expand_ref,
    project_ref,
    gqt_ref, gw_ref, flat1_ref, flat2_ref, rows_ref,
    q_ref, v_ref, kt_ref, p_ref, scale_ref, o_ref, ot_ref, a1t_ref, h1_ref, a2_ref, a2t_ref,
    own0_ref, ownw_ref, own1_ref, own2_ref, square_ref, vec_ref,
    all0_ref, allw_ref, w1_ref, w2_ref, vecs_ref, bqv_ref, x_ref, a1_ref, k_ref, qt_ref, vt_ref,
    send_sem, recv_sem, local_sem,
):
    t = pl.program_id(0)
    n, _ = x_ref.shape
    width = allw_ref.shape[-1]
    heads = width // HEAD_DIM
    step = 256
    place = Place()
    length = len_ref[place.t]
    links = Links(send_sem, recv_sem)
    z, y, x, c = place.z, place.y, place.x, place.c
    mine_there = vecs_ref.at[z, y, x, c]
    column = vecs_ref.at[:, :, x, c]
    vec_one = [links.add(device, vec_ref, mine_there) for device in place.same_t]
    vec_two = [links.add(device, column, column) for device in place.same_dp]
    seg0 = Gather(
        links, place, own0_ref, lambda k, z, y: all0_ref.at[k, z, y], Z_Y_X, single=False
    )
    segw = Gather(links, place, ownw_ref, lambda k, z, y: allw_ref.at[k, z, y], Z_Y_X)
    seg1 = Gather(
        links, place, own1_ref, lambda k, z, y: w1_ref.at[k, z, y], Y_Z_X, last=False
    )
    seg2 = Gather(
        links, place, own2_ref, lambda k, z, y: w2_ref.at[k, z, y], X_Z_Y, last=False
    )
    flush = [
        pltpu.make_async_copy(w1_ref, flat1_ref, local_sem.at[0]),
        pltpu.make_async_copy(w2_ref, flat2_ref, local_sem.at[1]),
    ]
    fetch = pltpu.make_async_copy(tokens_ref.at[place.t], x_ref, local_sem.at[2])

    def relay_z(copies):
        recv(copies[1])
        start(copies[2])

    def pass_own(seg):
        recv(seg.z[0], seg.z[2])
        if seg is segw:
            start(seg.first)
        start(seg.second[0], seg.core[0])

    def pass_first(seg):
        recv(seg.first)
        if seg is segw:
            start(seg.second[1], seg.core[1])
        else:
            start(seg.far[1], seg.far[0])

    def pass_far(seg):
        recv(seg.far[0], seg.far[2])
        start(seg.core[1])

    def pass_core(seg, i):
        recv(seg.second[i])
        start(seg.core[2 + i])

    plan = [
        (0, 0, lambda: (pass_own(segw), pass_first(seg1), relay_z(seg2.z), pass_first(seg2))),
        (0, 3, lambda: (pass_first(segw), relay_z(seg1.z), pass_core(seg0, 0))),
        (1, 0, lambda: recv(seg0.core[:2])),
        (1, 1, lambda: relay_z(seg1.far)),
        (1, 3, lambda: pass_core(seg0, 1)),
        (1, 4, lambda: (recv(segw.core[:2]), pass_core(segw, 0), pass_own(seg2))),
        (2, 1, lambda: relay_z(seg2.far)),
        (2, 2, lambda: pass_core(segw, 1)),
        (2, 3, lambda: pass_own(seg1)),
        (3, 0, lambda: (recv(seg0.core[2:]), pass_far(seg1))),
        (3, 2, lambda: (pass_far(seg2), pass_core(seg2, 0))),
        (3, 4, lambda: recv(segw.core[2:])),
    ]

    def serve(point):
        for step, where, act in plan:
            if where == point:
                pl.when(t == step)(lambda act=act: (act(), None)[1])

    @pl.when(t == 0)
    def _():
        s0, s1, s2, s3 = tie_ref[0], tie_ref[1], tie_ref[2], tie_ref[3]
        fetch.start()
        square_ref[...] = jnp.zeros_like(square_ref)
        gain = gains_ref.shape[-1]
        square_ref[0:1, :gain] = gains_ref[s0].astype(F32)[0:1]
        square_ref[1:2, :gain] = gains_ref[s2].astype(F32)[1:2]
        kinds = [s0, s0, s0, s1, s2, s3, s2, s2, s2, s2]
        for i, source in enumerate(kinds):
            wide = bias_ref[i].astype(F32)
            here = lax.broadcasted_iota(jnp.int32, wide.shape, 0) == source
            square_ref[2 + i : 3 + i, :gain] = jnp.sum(
                jnp.where(here, wide, 0.0), 0, keepdims=True
            )
        vec_ref[...] = square_ref[...].T[:gain]
        for j in range(3):
            own0_ref[:, j * width : (j + 1) * width] = in_ref[s0, j]
        place.greet(place.same_t + place.same_dp)
        start(vec_one, seg0.z[1], seg0.z[0], seg0.first[0])
        vecs_ref[z, y, x, c] = vec_ref[...]
        ones = lax.broadcasted_iota(jnp.int32, (vt_ref.shape[1] - HEAD_DIM, n), 0) == 0
        for h in range(heads):
            vt_ref[h, HEAD_DIM:, :] = ones.astype(BF16)
        all0_ref[0, z, y] = own0_ref[...]
        ownw_ref[...] = out_ref[s1].T
        allw_ref[0, z, y] = ownw_ref[...]
        own1_ref[...] = expand_ref[s2]
        own2_ref[...] = project_ref[s3]
        w1_ref[0, z, y] = own1_ref[...]
        w2_ref[0, z, y] = own2_ref[...]
        recv(vec_one)
        start(vec_two)
        relay_z(seg0.z)
        start(seg0.first[2])
        recv(seg0.z[0])
        start(seg0.first[1], segw.z[1], segw.z[0], seg2.z[1])
        recv(vec_two)
        start(seg2.first)
        vecs = vecs_ref[...].reshape(D, vecs_ref.shape[-1]).T[:16]
        rows_ref[...] = vecs
        recv(seg0.z[2])
        start(seg0.first[3], seg1.first, seg0.second[0], seg0.core[0])
        for k in range(4):
            part = slice(k * width, (k + 1) * width)
            bqv_ref[k, 0:1, :width] = vecs[3:4, part]
            bqv_ref[k, 0:1, width : 2 * width] = jnp.zeros((1, width), F32)
            bqv_ref[k, 0:1, 2 * width :] = vecs[4:5, part]
        fetch.wait()

        @pl.loop(0, n // step)
        def _(b):
            rows = pl.ds(pl.multiple_of(b * step, step), step)
            wide = x_ref[rows, :].astype(F32)
            xhat, _ = norm_parts(wide)
            a1 = (xhat * rows_ref[0:1, :] + rows_ref[2:3, :]).astype(BF16)
            a1_ref[rows, :] = a1
            a1t_ref[:, rows] = a1.T
            h1_ref[rows, :] = wide + rows_ref[5:6, :]

        relay_z(segw.z)
        start(seg2.z[0], seg1.z[1], seg1.z[0])
        recv(seg0.first)
        start(seg0.second[1], seg0.core[1])

    serve(0)
    gq = all0_ref[t].reshape(D, 3 * width)
    gqt_ref[0] = gq.T
    mine = place.group(t)
    qkv = dot_nn(a1_ref[...], gq) + bqv_ref[mine, 0:1, :]
    q = qkv[:, :width].astype(BF16) * jnp.asarray(HEAD_DIM ** -0.5, BF16)
    k = qkv[:, width : 2 * width].astype(BF16)
    v = qkv[:, 2 * width :].astype(BF16)
    q_ref[0] = q
    kt_ref[0] = k.T
    v_ref[0] = v
    vt = v.T
    for h in range(heads):
        vt_ref[h, :HEAD_DIM, :] = vt[h * HEAD_DIM : (h + 1) * HEAD_DIM]
    spare = k_ref.shape[1] - width
    dead = lax.broadcasted_iota(jnp.int32, (n, spare), 0) >= length
    first_column = lax.broadcasted_iota(jnp.int32, (n, spare), 1) == 0
    first_row = lax.broadcasted_iota(jnp.int32, (spare, n), 0) == 0
    k_ref[:, :width] = k
    k_ref[:, width:] = jnp.where(first_column & dead, MASKED, 0.0).astype(BF16)
    qt_ref[:width, :] = q.T
    qt_ref[width:, :] = jnp.where(first_row, 1.0, 0.0).astype(BF16)

    serve(1)
    def scores(h, b):
        first, last = b * step, (b + 1) * step
        qt = qt_ref[:, first:last]
        row = lax.broadcasted_iota(jnp.int32, (qt.shape[0], 1), 0)
        keep = ((row >= h * HEAD_DIM) & (row < (h + 1) * HEAD_DIM)) | (row >= width)
        return dot_nn(k_ref[:last, :], jnp.where(keep, qt, jnp.zeros((), BF16)))

    def attend(h, b, s):
        first, last = b * step, (b + 1) * step
        key = lax.broadcasted_iota(jnp.int32, (step, step), 0)
        query = lax.broadcasted_iota(jnp.int32, (step, step), 1)
        near = jnp.where(key <= query, s[first:], MASKED)
        top = jnp.max(near, 0, keepdims=True)
        if b:
            far = s[:first]
            top = jnp.maximum(top, jnp.max(far, 0, keepdims=True))
        e_near = jnp.exp((near - top).astype(BF16))
        p_ref[0, h, first:last, first:last] = e_near
        o = dot_nn(vt_ref[h, :, first:last], e_near)
        if b:
            e_far = jnp.exp((far - top).astype(BF16))
            p_ref[0, h, :first, first:last] = e_far
            o += dot_nn(vt_ref[h, :, :first], e_far)
        scale = 1.0 / o[HEAD_DIM : HEAD_DIM + 1]
        scale_ref[0, h : h + 1, first:last] = scale
        ot_ref[0, h * HEAD_DIM : (h + 1) * HEAD_DIM, first:last] = (
            o[:HEAD_DIM] * scale
        ).astype(BF16)

    scale_ref[0, heads:, :] = jnp.zeros((scale_ref.shape[1] - heads, n), F32)
    for h in range(heads):
        s = scores(h, 0)
        for b in range(n // step):
            ahead = scores(h, b + 1) if b + 1 < n // step else None
            attend(h, b, s)
            s = ahead
        serve(2 + h)

    gw_ref[0] = allw_ref[t].reshape(gw_ref.shape[1:])
    o = ot_ref[0].T
    o_ref[0] = o
    h1_ref[...] += dot_nt(o, gw_ref[0])

    @pl.when(t == 3)
    def _():
        @pl.loop(0, n // step)
        def _(b):
            rows = pl.ds(pl.multiple_of(b * step, step), step)
            h1 = h1_ref[rows, :]
            xhat, _ = norm_parts(h1)
            a2 = (xhat * rows_ref[1:2, :] + rows_ref[6:7, :]).astype(BF16)
            a2_ref[rows, :] = a2
            a2t_ref[:, rows] = a2.T

        pass_core(seg1, 0)
        recv(seg2.core)
        flush[1].start()
        recv(seg1.core)
        flush[0].start()
        links.sent()
        for copy in flush:
            copy.wait()


N_GATHER = 10 + 13 + 10 + 11 + 11
VMEM_WHOLE = pl.BlockSpec(memory_space=pltpu.VMEM)
ANY_WHOLE = pl.BlockSpec(memory_space=pl.ANY)


def run_fused_forward(tie, lengths, tokens, gains, biases, w_in, w_out, w_expand, w_project):
    groups, n, _ = tokens.shape
    depth, width = w_in.shape[-2:]
    heads = width // HEAD_DIM
    hidden = w_expand.shape[-1]
    w_project = w_project.transpose(0, 2, 1)
    biases = biases.transpose(1, 0, 2)
    own = gains.shape[-1]
    return pl.pallas_call(
        fused_forward,
        grid=(groups,),
        in_specs=[SMEM_WHOLE, SMEM_WHOLE, ANY_WHOLE] + [VMEM_WHOLE] * 6,
        out_specs=[
            group(3 * width, D), group(D, width), ANY_WHOLE, ANY_WHOLE, VMEM_WHOLE,
            group(n, width), group(n, width), group(width, n), group(heads, n, n),
            group(8, n), group(n, width), group(width, n), VMEM_WHOLE, VMEM_WHOLE, VMEM_WHOLE, VMEM_WHOLE,
        ],
        out_shape=[
            shaped(BF16, groups, 3 * width, D), shaped(BF16, groups, D, width),
            shaped(BF16, groups, Z_DEV, Y_DEV, depth, hidden),
            shaped(BF16, groups, Z_DEV, Y_DEV, depth, hidden),
            shaped(F32, 16, D),
            shaped(BF16, groups, n, width), shaped(BF16, groups, n, width),
            shaped(BF16, groups, width, n), shaped(BF16, groups, heads, n, n),
            shaped(F32, groups, 8, n), shaped(BF16, groups, n, width),
            shaped(BF16, groups, width, n), shaped(BF16, D, n), shaped(F32, n, D),
            shaped(BF16, n, D), shaped(BF16, D, n),
        ],
        scratch_shapes=[
            pltpu.VMEM((depth, 3 * width), BF16), pltpu.VMEM((depth, width), BF16),
            pltpu.VMEM((depth, hidden), BF16), pltpu.VMEM((depth, hidden), BF16),
            pltpu.VMEM((128, 128), F32), pltpu.VMEM((own, 128), F32),
            pltpu.VMEM((groups, Z_DEV, Y_DEV, depth, 3 * width), BF16),
            pltpu.VMEM((groups, Z_DEV, Y_DEV, depth, width), BF16),
            pltpu.VMEM((groups, Z_DEV, Y_DEV, depth, hidden), BF16),
            pltpu.VMEM((groups, Z_DEV, Y_DEV, depth, hidden), BF16),
            pltpu.VMEM((Z_DEV, Y_DEV, X_DEV, C_DEV, own, 128), F32),
            pltpu.VMEM((groups, 8, 3 * width), F32),
            pltpu.VMEM((n, D), BF16), pltpu.VMEM((n, D), BF16), pltpu.VMEM((n, 256), BF16),
            pltpu.VMEM((256, n), BF16), pltpu.VMEM((heads, HEAD_DIM + 16, n), BF16),
            pltpu.SemaphoreType.DMA((N_GATHER,)), pltpu.SemaphoreType.DMA((N_GATHER,)),
            pltpu.SemaphoreType.DMA((3,)),
        ],
        compiler_params=pltpu.CompilerParams(
            vmem_limit_bytes=VMEM_LIMIT, collective_id=0, has_side_effects=True
        ),
        name="fused_forward",
    )(tie, lengths, tokens, gains, biases, w_in, w_out, w_expand, w_project)


class Result:
    def __init__(self, links, place, own_ref, passing_ref, out_ref, step, sem):
        count = own_ref.shape[0] // step
        self.own_ref, self.passing_ref, self.out_ref, self.sem = own_ref, passing_ref, out_ref, sem
        self.place = place
        self.x, self.core, self.far = [], [], []
        for i in range(count):
            rows = pl.ds(i * step, step)
            mine, theirs = out_ref.at[place.t, rows], out_ref.at[place.ts[2], rows]
            self.x.append(links.add(place.to_x, own_ref.at[rows], passing_ref.at[rows]))
            self.core.append(links.add(place.to_core, own_ref.at[rows], mine))
            self.far.append(links.add(place.to_core, passing_ref.at[rows], theirs))

    def send(self, i):
        start(self.x[i], self.core[i])

    def pass_on(self, i):
        recv(self.x[i])
        start(self.far[i])

    def finish(self):
        for ref, where in [
            (self.own_ref, self.place.t), (self.passing_ref, self.place.ts[2])
        ]:
            copy = pltpu.make_async_copy(ref, self.out_ref.at[where], self.sem)
            copy.start()
            copy.wait()
        recv(self.core, self.far)


def pair_order(i):
    return i + 1 - 2 * (i % 2)


def fused_feed_forward(
    len_ref, cot_ref, a2_ref, a2t_ref, h1_ref, far1_ref, far2_ref, rows_ref,
    out_ref, fold_ref, work_ref, dh1_ref, gb_ref, gbt_ref, sums_ref,
    gf_ref, gft_ref, feed_ref, da2_ref, h_ref, df_ref, weights_ref, turned_ref, missing_ref,
    stage_ref, land_ref, near_ref, cross_ref,
    send_sem, recv_sem, local_sem,
):
    t = pl.program_id(0)
    n = gf_ref.shape[0]
    step = 256
    depth = stage_ref.shape[-2]
    place = Place()
    length = len_ref[place.t]
    links = Links(send_sem, recv_sem)
    y, other = place.y, place.other_y
    last = [
        links.add(place.to_x, far1_ref.at[0, :, other], missing_ref.at[0, 0]),
        links.add(place.to_y, far2_ref.at[2, :, y], missing_ref.at[1, 0]),
    ]
    last_core = [
        links.add(place.to_core, missing_ref.at[i, 0], missing_ref.at[i, 1]) for i in range(2)
    ]
    core = [
        [links.add(place.to_core, stage_ref.at[i], land_ref.at[s, i]) for i in range(2)]
        for s in range(2)
    ]
    cross = [
        links.add(place.to_y, near_ref.at[i, :, other], cross_ref.at[i]) for i in range(2)
    ]
    fetch = pltpu.make_async_copy(cot_ref.at[place.t], gf_ref, local_sem.at[0])
    k = pair_order(t)
    mine = place.group(k)

    def load(step, whole, slot):
        for i, far_ref in enumerate([far1_ref, far2_ref]):
            group = far_ref.at[pair_order(step)]
            to = weights_ref.at[slot, i]
            if not whole:
                group, to = group.at[:, y], to.at[:, y]
            yield pltpu.make_async_copy(group, to, local_sem.at[1 + 2 * slot + i])

    def live_rows(b):
        at = b * step + lax.broadcasted_iota(jnp.int32, (step, 1), 0)
        return (at < length).astype(F32)

    @pl.when(t == 0)
    def _():
        fetch.start()
        for copy in load(0, True, 0):
            copy.start()
        place.greet()
        start(last)
        sums_ref[...] = jnp.zeros_like(sums_ref)
        feed_ref[...] = jnp.zeros_like(feed_ref)
        da2_ref[...] = jnp.zeros_like(da2_ref)
        fetch.wait()

        @pl.loop(0, n // step)
        def _(b):
            rows = pl.ds(pl.multiple_of(b * step, step), step)
            g = (gf_ref[rows, :].astype(F32) * live_rows(b)).astype(BF16)
            gf_ref[rows, :] = g
            gft_ref[:, rows] = g.T
            sums_ref[7:8, :] += jnp.sum(g.astype(F32), 0, keepdims=True)

    for i in range(4):
        @pl.when(t == i)
        def _():
            if i == 2:
                recv(last_core)
            for copy in load(i, i < 2, i % 2):
                copy.wait()
            if i < 3:
                for copy in load(i + 1, i + 1 < 2, (i + 1) % 2):
                    copy.start()
            if i >= 2:
                for j in range(2):
                    weights_ref[i % 2, j, :, other] = missing_ref[j, 3 - i]

    for i in range(2):
        turned_ref[i] = weights_ref[t % 2, i].reshape(D, -1).T

    bias = rows_ref[pl.ds(8 + mine, 1), :]
    w1 = weights_ref[t % 2, 0].reshape(D, -1)
    w2 = weights_ref[t % 2, 1].reshape(D, -1)
    column = jnp.zeros((1, w1.shape[1]), F32)
    for rows in blocks(n, 2 * step):
        f = dot_nn(a2_ref[rows, :], w1) + bias
        dh = dot_nn(gf_ref[rows, :], w2)
        f2 = f * f
        th = jnp.tanh(f * (SQRT_2_PI + (SQRT_2_PI * 0.044715) * f2))
        half = 0.5 + 0.5 * th
        h = (f * half).astype(BF16)
        slope = half + f * (0.5 - 0.5 * th * th) * (
            SQRT_2_PI + (3 * SQRT_2_PI * 0.044715) * f2
        )
        df = (dh * slope).astype(BF16)
        h_ref[rows, :] = h
        df_ref[rows, :] = df
        column += jnp.sum(df.astype(F32), 0, keepdims=True)
        feed_ref[rows, :] += dot_nn(h, turned_ref[1])
        da2_ref[rows, :] += dot_nn(df, turned_ref[0])
    sums_ref[pl.ds(8 + mine, 1), :] = column

    @pl.when(t == 1)
    def _():
        recv(last)
        start(last_core)

    def weight_grad(left_ref, right_ref):
        value = dot_nn(left_ref[...], right_ref[...])
        return value.reshape(Z_DEV, Y_DEV, depth, value.shape[-1]).astype(BF16)

    grad1 = weight_grad(a2t_ref, df_ref)
    grad2 = weight_grad(gft_ref, h_ref)

    def put(ref):
        ref[0] = grad1
        ref[1] = grad2

    def reduced(ref):
        return lambda i, s, z: (
            ref[i, z].astype(F32) + land_ref[s, i, z].astype(F32)
        ).astype(BF16)

    @pl.when(t == 0)
    def _():
        put(stage_ref)
        start(core[0])

    @pl.when(t == 1)
    def _():
        put(near_ref)
        recv(core[0])

        @pl.loop(0, Z_DEV)
        def _(z):
            for i in range(2):
                near_ref[i, z] = reduced(near_ref)(i, 0, z)

        start(cross)

    @pl.when(t == 2)
    def _():
        for copy in core[0]:
            copy.wait_send()
        put(stage_ref)
        start(core[1])

    @pl.when(t == 3)
    def _():
        put(work_ref)

        @pl.loop(0, n // step)
        def _(b):
            rows = pl.ds(pl.multiple_of(b * step, step), step)
            live = live_rows(b)
            h1 = h1_ref[rows, :]
            out_ref[rows, :] = (live * (h1 + (feed_ref[rows, :] + rows_ref[7:8, :]))).astype(BF16)
            xhat, r = norm_parts(h1)
            da2 = da2_ref[rows, :]
            sums_ref[1:2, :] += jnp.sum(da2 * xhat, 0, keepdims=True)
            sums_ref[6:7, :] += jnp.sum(da2, 0, keepdims=True)
            dg = da2 * rows_ref[1:2, :]
            dv = r * (
                dg
                - jnp.mean(dg, -1, keepdims=True)
                - xhat * jnp.mean(dg * xhat, -1, keepdims=True)
            )
            dh1 = gf_ref[rows, :].astype(F32) + dv
            dh1_ref[rows, :] = dh1
            gb = dh1.astype(BF16)
            gb_ref[rows, :] = gb
            gbt_ref[:, rows] = gb.T
            sums_ref[5:6, :] += jnp.sum(gb.astype(F32), 0, keepdims=True)

        recv(core[1])

        @pl.loop(0, Z_DEV)
        def _(z):
            for i in range(2):
                work_ref[i, z] = reduced(work_ref)(i, 1, z)

        recv(cross)

        @pl.loop(0, Z_DEV)
        def _(z):
            for i in range(2):
                fold_ref[i, z] = (
                    near_ref[i, z, y].astype(F32) + cross_ref[i, z].astype(F32)
                ).astype(BF16)

        links.sent(*core[0])


def run_fused_feed_forward(lengths, cot, a2, a2t, h1, g1, g2, rows):
    n = cot.shape[1]
    groups, _, _, depth, hidden = g1.shape
    both = (2, Z_DEV, Y_DEV, depth, hidden)
    fold = (2, Z_DEV, depth, hidden)
    return pl.pallas_call(
        fused_feed_forward,
        grid=(groups,),
        in_specs=[SMEM_WHOLE, ANY_WHOLE] + [VMEM_WHOLE] * 3 + [ANY_WHOLE] * 2
        + [VMEM_WHOLE],
        out_specs=[VMEM_WHOLE] * 7,
        out_shape=[
            shaped(BF16, n, D), shaped(BF16, *fold), shaped(BF16, *both), shaped(F32, n, D),
            shaped(BF16, n, D), shaped(BF16, D, n), shaped(F32, 16, D),
        ],
        scratch_shapes=[
            pltpu.VMEM((n, D), BF16), pltpu.VMEM((D, n), BF16), pltpu.VMEM((n, D), F32),
            pltpu.VMEM((n, D), F32), pltpu.VMEM((n, hidden), BF16), pltpu.VMEM((n, hidden), BF16),
            pltpu.VMEM((2,) + both, BF16), pltpu.VMEM((2, hidden, D), BF16),
            pltpu.VMEM((2,) + fold, BF16), pltpu.VMEM(both, BF16), pltpu.VMEM((2,) + both, BF16),
            pltpu.VMEM(both, BF16), pltpu.VMEM(fold, BF16),
            pltpu.SemaphoreType.DMA((10,)), pltpu.SemaphoreType.DMA((10,)),
            pltpu.SemaphoreType.DMA((5,)),
        ],
        compiler_params=pltpu.CompilerParams(
            vmem_limit_bytes=VMEM_LIMIT, collective_id=1, has_side_effects=True
        ),
        name="fused_feed_forward",
    )(lengths, cot, a2, a2t, h1, g1, g2, rows)
class Reduce:
    def __init__(
        self, links, place, work, acc, cross_ref, far_ref, mid_ref, last_ref, side_ref,
        slots=(0, 1),
    ):
        self.place, self.work, self.acc = place, work, acc
        self.cross_ref, self.far_ref, self.mid_ref = cross_ref, far_ref, mid_ref
        self.last_ref, self.side_ref = last_ref, side_ref
        zs = place.zs
        self.y = {
            s: [
                links.add(place.to_y, work(s, zs[j], place.other_y), cross_ref.at[s, zs[j]])
                for j in (1, 3, 2, 0)
            ]
            for s in slots
        }
        self.z = [
            [
                links.add(place.to_z[1], acc(s, zs[1]), far_ref.at[s, 0]),
                links.add(place.to_z[1], acc(s, zs[3]), far_ref.at[s, 1]),
                links.add(place.to_z[2], mid_ref.at[s, 1], far_ref.at[s, 2]),
            ]
            for s in range(2)
        ]
        self.x = links.add(place.to_x, last_ref, side_ref)

    def fold_y(self, s, half):
        for i, j in [(0, 1), (1, 3), (2, 2), (3, 0)][2 * half : 2 * half + 2]:
            z = self.place.zs[j]
            recv(self.y[s][i])
            value = self.work(s, z, self.place.y)[...].astype(F32)
            self.acc(s, z)[...] = (value + self.cross_ref[s, z].astype(F32)).astype(BF16)
            if i < 2:
                start(self.z[s][i])

    def fold_z(self, s):
        recv(self.z[s][:2])
        for i in (1, 0):
            value = self.acc(s, self.place.zs[2 * i])[...].astype(F32)
            self.mid_ref[s, i] = (value + self.far_ref[s, i].astype(F32)).astype(BF16)
            if i:
                start(self.z[s][2])

    def own(self, s):
        recv(self.z[s][2])
        return self.mid_ref[s, 0].astype(F32) + self.far_ref[s, 2].astype(F32)

    def send_x(self):
        self.last_ref[...] = self.own(1).astype(BF16)
        start(self.x)

    def total(self):
        value = self.own(0)
        recv(self.x)
        return value + self.side_ref[...].astype(F32)


def fused_backward(
    tokens_ref, gqt_ref, gw_ref, rows_ref, dh1_ref, gb_ref, gbt_ref, q_ref, v_ref, kt_ref,
    p_ref, scale_ref, o_ref, ot_ref, a1t_ref, layer_ref, fold_ref, work_ref, early_ref,
    out_ref, layerout_ref, part0_ref, partw_ref, part1_ref, part2_ref, total_ref,
    do_ref, dot_ref, delta_ref, dkv_ref, dqkv_ref, da1_ref, own_ref, passing_ref, passlayer_ref, bqv_ref,
    folded_ref, cross1_ref, far1_ref, mid1_ref, last1_ref, side1_ref,
    cross2_ref, far2_ref, mid2_ref, last2_ref, side2_ref,
    stagew_ref, landw_ref, workw_ref, crossw_ref, farw_ref, midw_ref, lastw_ref, sidew_ref,
    stage0_ref, land0_ref, work0_ref, cross0_ref, far0_ref, mid0_ref, last0_ref, side0_ref,
    sums_ref, sumland_ref,
    send_sem, recv_sem, local_sem,
):
    t = pl.program_id(0)
    n = own_ref.shape[0]
    width = gw_ref.shape[-1]
    depth = part0_ref.shape[0]
    heads = width // HEAD_DIM
    step = n // 4
    place = Place()
    y = place.y
    links = Links(send_sem, recv_sem)
    k, i = group_and_block(t)
    mine = place.group(k)
    now = k % 2
    out = Result(links, place, own_ref, passing_ref, out_ref, step, local_sem.at[0])
    layer = Result(links, place, layer_ref, passlayer_ref, layerout_ref, step, local_sem.at[1])
    fetch = pltpu.make_async_copy(tokens_ref.at[place.t], own_ref, local_sem.at[2])
    corew = [links.add(place.to_core, stagew_ref, landw_ref.at[i]) for i in range(2)]
    core0 = [links.add(place.to_core, stage0_ref, land0_ref.at[i]) for i in range(2)]
    def half_done(i, *landing):
        return Reduce(
            links, place, lambda s, z, y: work_ref.at[i, z, y],
            lambda s, z: folded_ref.at[i, z] if s else fold_ref.at[i, z],
            *landing, slots=(1,),
        )

    seg1 = half_done(0, cross1_ref, far1_ref, mid1_ref, last1_ref, side1_ref)
    seg2 = half_done(1, cross2_ref, far2_ref, mid2_ref, last2_ref, side2_ref)
    segw = Reduce(
        links, place, lambda s, z, y: workw_ref.at[s, z, y],
        lambda s, z: workw_ref.at[s, z, y],
        crossw_ref, farw_ref, midw_ref, lastw_ref, sidew_ref,
    )
    seg0 = Reduce(
        links, place, lambda s, z, y: work0_ref.at[s, z, y],
        lambda s, z: work0_ref.at[s, z, y],
        cross0_ref, far0_ref, mid0_ref, last0_ref, side0_ref,
    )
    sum_core, sum_y, *sum_z, sum_x = [
        links.add(to, sums_ref.at[i], sumland_ref.at[j])
        for j, (i, to) in enumerate(
            zip([0, 1, 2, 2, 2, 3], [place.to_core, place.to_y] + place.to_z[1:] + [place.to_x])
        )
    ]

    def when(point):
        return pl.when(t == point)

    @when(0)
    def _():
        fetch.start()
        place.greet()
        for i in range(4):
            layer.send(i)
        start(seg1.y[1], seg2.y[1])
        start(seg1.z[0][:2], seg2.z[0][:2])
        bqv_ref[...] = jnp.zeros_like(bqv_ref)
        sums_ref[0] = early_ref[...]
        da1_ref[...] = jnp.zeros_like(da1_ref)
        fetch.wait()

    def add_core():
        recv(corew[1])

        @pl.loop(0, Z_DEV)
        def _(z):
            workw_ref[1, z] = (
                workw_ref[1, z].astype(F32) + landw_ref[1, z].astype(F32)
            ).astype(BF16)

        start(segw.y[1])

    plan = [
        (2, 1, lambda: (seg1.fold_y(1, 0), seg1.fold_z(0))),
        (3, 1, lambda: layer.pass_on(0)),
        (4, 0, lambda: (seg1.fold_y(1, 1), seg2.fold_z(0))),
        (4, 1, lambda: layer.pass_on(1)),
        (5, 1, lambda: (seg1.fold_z(1), seg2.fold_y(1, 0))),
        (8, 0, lambda: (seg2.fold_y(1, 1), layer.pass_on(2))),
        (8, 1, lambda: (seg1.send_x(), segw.fold_y(0, 0), segw.fold_y(0, 1))),
        (9, 0, add_core),
        (9, 1, lambda: (seg2.fold_z(1), seg0.fold_y(0, 0), layer.pass_on(3))),
        (10, 1, lambda: segw.fold_z(0)),
        (11, 1, lambda: (seg2.send_x(), seg0.fold_y(0, 1))),
        (12, 1, lambda: (segw.fold_y(1, 0), segw.fold_y(1, 1))),
        (13, 1, lambda: (seg0.fold_z(0), out.pass_on(3))),
        (14, 1, lambda: segw.fold_z(1)),
    ]

    def serve(point):
        for at, where, act in plan:
            if where == point:
                pl.when(t == at)(lambda act=act: (act(), None)[1])

    @pl.when((t == 0) | (t == 4) | (t == 8) | (t == 9))
    def _():
        @pl.loop(0, n // step)
        def _(i):
            rows = pl.ds(pl.multiple_of(i * step, step), step)
            columns = scale_ref[0, :, rows].T
            lane = lax.broadcasted_iota(jnp.int32, (step, width), 1)
            scale = columns[:, heads - 1 : heads]
            for h in reversed(range(heads - 1)):
                scale = jnp.where(lane < (h + 1) * HEAD_DIM, columns[:, h : h + 1], scale)
            do = (dot_nn(gb_ref[rows, :], gw_ref[0]) * scale).astype(BF16)
            do_ref[now, rows, :] = do
            dot = do.T
            dot_ref[now, :, rows] = dot
            product = dot.astype(F32) * ot_ref[0, :, rows].astype(F32)
            for h in range(heads):
                head = slice(h * HEAD_DIM, (h + 1) * HEAD_DIM)
                delta_ref[now, h : h + 1, rows] = jnp.sum(product[head], 0, keepdims=True)

        value = dot_nn(gbt_ref[...], o_ref[0]).reshape(Z_DEV, Y_DEV, depth, width)
        for s in range(2):
            @when(8 * s)
            def _():
                if s:
                    corew[0].wait_send()
                stagew_ref[...] = value.astype(BF16)
                start(corew[s])

        @when(4)
        def _():
            recv(corew[0])
            workw_ref[0] = (value + landw_ref[0].astype(F32)).astype(BF16)
            start(segw.y[0])

        @when(9)
        def _():
            workw_ref[1] = value.astype(BF16)

    serve(0)

    for ii in reversed(range(4)):
        @pl.when(i == ii)
        def _():
            first, last = ii * step, (ii + 1) * step
            do = do_ref[now, first:last, :]
            dot = dot_ref[now, :, first:last]
            q = q_ref[0, first:last, :]
            v = v_ref[0, :last, :]
            row = lax.broadcasted_iota(jnp.int32, (width, 1), 0)
            lane = lax.broadcasted_iota(jnp.int32, (1, width), 1)
            dk, dv, dq = None, None, []
            for h in range(heads):
                low, high = h * HEAD_DIM, (h + 1) * HEAD_DIM
                here = (row >= low) & (row < high)
                p = p_ref[0, h, :last, :]
                dp = dot_nn(v, jnp.where(here, dot, jnp.zeros((), BF16)))
                ds = p * (dp - delta_ref[now, h : h + 1, first:last]).astype(BF16)
                part = dot_nn(p, do)
                dv = part if dv is None else jnp.where(lane < low, dv, part)
                part = dot_nn(ds, q)
                dk = part if dk is None else jnp.where(lane < low, dk, part)
                dq.append(dot_nn(kt_ref[0, low:high, :last], ds))
            if ii == 3:
                dkv_ref[now, 0] = dk
                dkv_ref[now, 1] = dv
            else:
                dkv_ref[now, 0, :last, :] += dk
                dkv_ref[now, 1, :last, :] += dv
            dk = dkv_ref[now, 0, first:last, :].astype(BF16)
            dv = dkv_ref[now, 1, first:last, :].astype(BF16)
            dq = (jnp.concatenate(dq, 0) * HEAD_DIM ** -0.5).astype(BF16).T
            dqkv_ref[now, first:last, :width] = dq
            dqkv_ref[now, first:last, width : 2 * width] = dk
            dqkv_ref[now, first:last, 2 * width :] = dv
            bqv_ref[mine, 0:1, :] += jnp.sum(dq.astype(F32), 0, keepdims=True)
            bqv_ref[mine, 1:2, :] += jnp.sum(dv.astype(F32), 0, keepdims=True)
            da1_ref[first:last, :] += dot_nn(dqkv_ref[now, first:last, :], gqt_ref[0])

    serve(1)

    @pl.when((t > 8) & (t % 2 == 1))
    def _():
        rows = pl.ds(pl.multiple_of(i * step, step), step)
        xhat, r = norm_parts(own_ref[rows, :].astype(F32))
        da1 = da1_ref[rows, :]
        sums_ref[0, 0:1, :] += jnp.sum(da1 * xhat, 0, keepdims=True)
        sums_ref[0, 2:3, :] += jnp.sum(da1, 0, keepdims=True)
        dg = da1 * rows_ref[0:1, :]
        dv = r * (
            dg
            - jnp.mean(dg, -1, keepdims=True)
            - xhat * jnp.mean(dg * xhat, -1, keepdims=True)
        )
        own_ref[rows, :] = (dh1_ref[...] + dv).astype(BF16)
        for ii in range(4):
            @pl.when(i == ii)
            def _():
                out.send(ii)

    @pl.when((t == 3) | (t == 7) | (t > 13))
    def _():
        value = dot_nn(a1t_ref[...], dqkv_ref[now]).reshape(Z_DEV, Y_DEV, depth, 3 * width)
        for s in range(2):
            @when(3 + 11 * s)
            def _():
                if s:
                    core0[0].wait_send()
                stage0_ref[...] = value.astype(BF16)
                start(core0[s])

            @when(7 + 8 * s)
            def _():
                recv(core0[s])
                work0_ref[s] = (value + land0_ref[s].astype(F32)).astype(BF16)
                start(seg0.y[s])

    @when(15)
    def _():
        for s in range(4):
            sums_ref[0, 3:5, s * width : (s + 1) * width] = bqv_ref[s, 0:2, :]
        start(sum_core)
        segw.send_x()
        out.pass_on(2)
        recv(sum_core)
        sums_ref[1] = sums_ref[0] + sumland_ref[0]
        start(sum_y)
        seg0.fold_y(1, 0)
        out.pass_on(1)
        seg0.fold_y(1, 1)
        recv(sum_y)
        sums_ref[2] = sums_ref[1] + sumland_ref[1]
        start(sum_z)
        seg0.fold_z(1)
        recv(sum_z)
        sums_ref[3] = (sums_ref[2] + sumland_ref[2]) + (sumland_ref[3] + sumland_ref[4])
        start(sum_x)
        part1_ref[...] = seg1.total()
        part2_ref[...] = seg2.total()
        seg0.send_x()
        partw_ref[...] = segw.total()
        layer.finish()
        out.pass_on(0)
        recv(sum_x)
        total_ref[...] = sums_ref[3] + sumland_ref[5]
        part0_ref[...] = seg0.total()
        out.finish()
        links.sent(corew[0], core0[0])


def group_and_block(t):
    early = t < 8
    return (
        jnp.where(early, 1 - t // 4, 3 - t % 2),
        3 - jnp.where(early, t % 4, jnp.maximum(t - 8, 0) // 2),
    )


def run_fused_backward(
    tokens, gqt, gw, rows, dh1, gb, gbt, q, v, kt, p, scale, o, ot, a1t, layer, fold, work,
    early,
):
    groups, n, _ = tokens.shape
    width = gw.shape[-1]
    heads = width // HEAD_DIM
    hidden = fold.shape[-1]
    depth = D // (Z_DEV * Y_DEV)
    step = n // 4

    def by_group(*shape):
        return pl.BlockSpec(
            (1,) + shape, lambda t: (group_and_block(t)[0],) + (0,) * len(shape)
        )

    p_spec = pl.BlockSpec(
        (1, heads, n, step),
        lambda t: (group_and_block(t)[0], 0, 0, group_and_block(t)[1]),
    )

    def early_group(*shape):
        return pl.BlockSpec(
            (1,) + shape, lambda t: (group_and_block(jnp.minimum(t, 9))[0],) + (0,) * len(shape)
        )

    copies = 2 * 12 + 4 + 2 * 15 + 2 * 11 + 6

    def landing(lanes):
        return [
            pltpu.VMEM((2, Z_DEV, depth, lanes), BF16),
            pltpu.VMEM((2, 3, depth, lanes), BF16), pltpu.VMEM((2, 2, depth, lanes), BF16),
            pltpu.VMEM((depth, lanes), BF16), pltpu.VMEM((depth, lanes), BF16),
        ]

    def working(lanes):
        block = (Z_DEV, Y_DEV, depth, lanes)
        return [pltpu.VMEM(block, BF16)] + [pltpu.VMEM((2,) + block, BF16)] * 2

    return pl.pallas_call(
        fused_backward,
        grid=(4 * groups,),
        in_specs=[
            ANY_WHOLE, by_group(3 * width, D), early_group(D, width), VMEM_WHOLE,
            pl.BlockSpec((step, D), lambda t: (group_and_block(jnp.maximum(t, 8))[1], 0)),
            VMEM_WHOLE, VMEM_WHOLE, by_group(n, width), by_group(n, width),
            by_group(width, n), p_spec, early_group(8, n), early_group(n, width),
            early_group(width, n),
            VMEM_WHOLE, VMEM_WHOLE, VMEM_WHOLE, VMEM_WHOLE, VMEM_WHOLE,
        ],
        out_specs=[ANY_WHOLE] * 2 + [VMEM_WHOLE] * 5,
        out_shape=[
            shaped(BF16, groups, n, D), shaped(BF16, groups, n, D),
            shaped(F32, depth, 3 * width),
            shaped(F32, depth, width), shaped(F32, depth, hidden),
            shaped(F32, depth, hidden), shaped(F32, 16, D),
        ],
        scratch_shapes=[
            pltpu.VMEM((2, n, width), BF16), pltpu.VMEM((2, width, n), BF16),
            pltpu.VMEM((2, 8, n), F32), pltpu.VMEM((2, 2, n, width), F32),
            pltpu.VMEM((2, n, 3 * width), BF16), pltpu.VMEM((n, D), F32),
            pltpu.VMEM((n, D), BF16), pltpu.VMEM((n, D), BF16), pltpu.VMEM((n, D), BF16),
            pltpu.VMEM((groups, 8, width), F32),
        ]
        + landing(hidden)[:1] + landing(hidden) + landing(hidden)
        + working(width) + landing(width)
        + working(3 * width) + landing(3 * width)
        + [
            pltpu.VMEM((4, 16, D), F32), pltpu.VMEM((6, 16, D), F32),
            pltpu.SemaphoreType.DMA((copies,)), pltpu.SemaphoreType.DMA((copies,)),
            pltpu.SemaphoreType.DMA((3,)),
        ],
        compiler_params=pltpu.CompilerParams(
            vmem_limit_bytes=VMEM_LIMIT, collective_id=2, has_side_effects=True
        ),
        name="fused_backward",
    )(
        tokens, gqt, gw, rows, dh1, gb, gbt, q, v, kt, p, scale, o, ot, a1t, layer, fold, work,
        early,
    )


def place_gradients(
    tie_ref, sums_ref, part0_ref, partw_ref, part1_ref, part2_ref, near_out_ref,
    near_grad_ref, far_out_ref, far_grad_ref, gains_ref, bias_ref, in_ref, out_ref, expand_ref,
    project_ref, held_ref, in_sem, out_sem,
):
    pairs = [(near_out_ref, far_out_ref), (near_grad_ref, far_grad_ref)]
    copies = []
    for i, (near_ref, far_ref) in enumerate(pairs):
        for j in range(near_ref.shape[0]):
            here = held_ref.at[i, j]
            copies.append((
                pltpu.make_async_copy(near_ref.at[j], here, in_sem.at[i, j]),
                pltpu.make_async_copy(here, far_ref.at[j], out_sem.at[i, j]),
            ))
    for fetch, _ in copies:
        fetch.start()
    own = gains_ref.shape[-1]
    width = partw_ref.shape[-1]
    first = (lax.axis_index("dp") * 4 + lax.axis_index("tensor")) * own
    feature = lax.broadcasted_iota(jnp.int32, (D, 128), 0)
    lane = lax.broadcasted_iota(jnp.int32, (D, 128), 1)
    chosen = ((feature == first + lane) & (lane < own)).astype(F32)
    sums = lax.dot_general(
        sums_ref[...], chosen, (((1,), (0,)), ((), ())),
        precision=lax.Precision.HIGHEST, preferred_element_type=F32,
    )[:, :own]
    s0, s1, s2, s3 = tie_ref[0], tie_ref[1], tie_ref[2], tie_ref[3]
    w_out = partw_ref[...].T

    def at(source, wanted, value):
        return jnp.where(source == wanted, value, jnp.zeros_like(value))

    row = lax.broadcasted_iota(jnp.int32, (NSRC, own), 0)
    for i, wanted in enumerate([s0, s0, s0, s1, s2, s3, s2, s2, s2, s2]):
        bias_ref[i] = jnp.where(row == wanted, sums[2 + i : 3 + i], 0.0)
    for s in range(NSRC):
        gains_ref[s, 0:1] = at(s, s0, sums[0:1])
        gains_ref[s, 1:2] = at(s, s2, sums[1:2])
        for j in range(3):
            in_ref[s, j] = at(s, s0, part0_ref[:, j * width : (j + 1) * width])
        out_ref[s] = at(s, s1, w_out)
        expand_ref[s] = at(s, s2, part1_ref[...])
        project_ref[s] = at(s, s3, part2_ref[...])
    for fetch, put in copies:
        fetch.wait()
        put.start()
    for _, put in copies:
        put.wait()


def run_place_gradients(tie, sums, part0, partw, part1, part2, out, grad, like):
    slots, n, _ = grad.shape
    gains, biases, w_in, w_out, w_expand, w_project = [item.shape for item in like]
    shapes = [
        gains, (biases[1], biases[0], biases[2]), w_in, w_out, w_expand,
        (w_project[0], w_project[2], w_project[1]),
    ]
    out, grad, gains, biases, w_in, w_out, w_expand, w_project = pl.pallas_call(
        place_gradients,
        in_specs=[SMEM_WHOLE] + [VMEM_WHOLE] * 5 + [ANY_WHOLE] * 2,
        out_specs=[ANY_WHOLE] * 2 + [VMEM_WHOLE] * 6,
        scratch_shapes=[
            pltpu.VMEM((2, slots, n, D), BF16),
            pltpu.SemaphoreType.DMA((2, slots)), pltpu.SemaphoreType.DMA((2, slots)),
        ],
        out_shape=[shaped(BF16, slots, n, D)] * 2 + [shaped(F32, *item) for item in shapes],
        compiler_params=pltpu.CompilerParams(vmem_limit_bytes=VMEM_LIMIT),
        name="place_gradients",
    )(tie, sums, part0, partw, part1, part2, out, grad)
    biases = biases.transpose(1, 0, 2)
    return out, grad, gains, biases, w_in, w_out, w_expand, w_project.transpose(0, 2, 1)


def plain_step(
    tokens, lengths, tie_map, norm_gains, bias_rows, attention_in, attention_out,
    expand_weight, project_weight, cotangent,
):
    slot_rows = tokens.shape[0] // lengths.shape[0]
    me = lax.axis_index("tensor")
    in_local = lax.dynamic_index_in_dim(attention_in, tie_map[0], 0, keepdims=False)
    out_local = lax.dynamic_index_in_dim(attention_out, tie_map[1], 0, keepdims=False)
    expand_local = lax.dynamic_index_in_dim(expand_weight, tie_map[2], 0, keepdims=False)
    project_local = lax.dynamic_index_in_dim(project_weight, tie_map[3], 0, keepdims=False)
    local0 = jnp.concatenate([in_local, out_local.T[None]], 0)
    row_kinds = jnp.array([0, 0, 0, 1, 2, 3] + [2] * (FF // D), dtype=jnp.int32)
    gain_kinds = jnp.array([0, 2], dtype=jnp.int32)
    gain_pick = norm_gains[tie_map[gain_kinds], jnp.arange(2)]
    bias_pick = bias_rows[tie_map[row_kinds], jnp.arange(row_kinds.shape[0])]
    vectors = jnp.concatenate([gain_pick, bias_pick], 0)
    x = lax.dynamic_slice_in_dim(tokens, me * slot_rows, slot_rows, 0)
    cot = lax.dynamic_slice_in_dim(cotangent, me * slot_rows, slot_rows, 0)
    length = lax.dynamic_slice_in_dim(lengths, me, 1, 0)
    rows = lax.all_gather(vectors, ("dp", "tensor"), axis=1, tiled=True).astype(F32)
    rows = jnp.concatenate([rows, jnp.zeros((4, D), F32)], 0)

    def gathered(piece, axis):
        piece = lax.all_gather(piece, "dp", axis=axis, tiled=True)
        return lax.all_gather(piece, "tensor", axis=0)

    g0 = gathered(local0, 1)
    g1 = gathered(expand_local, 0)
    g2 = gathered(project_local.T, 0)
    groups, width = g0.shape[0], g0.shape[-1]
    bqv = rows[3:5].reshape(2, groups, width).transpose(1, 0, 2)
    q, v, kt, p, o, a1t, h1, a2, a2t = run_attention_forward(length, x, g0, rows, bqv)
    out, d1, d2, dh1, gb, gbt, sums = run_feed_forward(length, cot, a2, a2t, h1, g1, g2, rows)
    d0, xg, sums_in, sums_qv = run_attention_backward(
        x, g0, rows, dh1, gb, gbt, q, v, kt, p, o, a1t
    )
    layer_out = lax.all_gather(out, "tensor", axis=0, tiled=True)
    tokens_grad = lax.all_gather(xg, "tensor", axis=0, tiled=True)

    def scattered(piece, axis):
        piece = lax.psum_scatter(piece, "tensor", scatter_dimension=0)
        return lax.psum_scatter(piece, "dp", scatter_dimension=axis, tiled=True).astype(F32)

    part0 = scattered(d0, 1)
    part1 = scattered(d1, 0)
    part2 = scattered(d2, 0)
    qv = sums_qv[:, :2].transpose(1, 0, 2).reshape(2, D)
    sums = jnp.concatenate(
        [sums_in[0:1], sums[1:2], sums_in[1:2], qv, sums[5:12]], 0
    )
    sums = lax.psum_scatter(sums, ("dp", "tensor"), scatter_dimension=1, tiled=True)
    return layer_out, tokens_grad, *placed(tie_map, sums, part0, part1, part2)


def fused_step(
    tokens, lengths, tie_map, norm_gains, bias_rows, attention_in, attention_out,
    expand_weight, project_weight, cotangent,
):
    slots = lengths.shape[0]
    tokens = tokens.reshape(slots, -1, D)
    cotangent = cotangent.reshape(slots, -1, D)
    gqt, gw, g1, g2, rows, q, v, kt, p, scale, o, ot, a1t, h1, a2, a2t = run_fused_forward(
        tie_map, lengths, tokens, norm_gains, bias_rows, attention_in, attention_out,
        expand_weight, project_weight,
    )
    layer, fold, work, dh1, gb, gbt, early = run_fused_feed_forward(
        lengths, cotangent, a2, a2t, h1, g1, g2, rows
    )
    grad, out, part0, partw, part1, part2, sums = run_fused_backward(
        tokens, gqt, gw, rows, dh1, gb, gbt, q, v, kt, p, scale, o, ot, a1t, layer, fold,
        work, early,
    )
    out, grad, *placed_grads = run_place_gradients(
        tie_map, sums, part0, partw, part1, part2, out, grad,
        (norm_gains, bias_rows, attention_in, attention_out, expand_weight, project_weight),
    )
    return out.reshape(-1, D), grad.reshape(-1, D), *placed_grads


def placed(tie_map, sums, part0, part1, part2):
    source = jnp.arange(NSRC, dtype=jnp.int32)

    def place(piece, which):
        pick = (source == tie_map[which]).reshape((NSRC,) + (1,) * piece.ndim)
        return jnp.where(pick, piece[None], 0.0)

    def place_rows(piece, kinds):
        pick = source[:, None] == tie_map[jnp.array(kinds, dtype=jnp.int32)][None, :]
        return jnp.where(pick[:, :, None], piece[None], 0.0)

    return (
        place_rows(sums[:2], [0, 2]),
        place_rows(sums[2:], [0, 0, 0, 1, 2, 3] + [2] * (FF // D)),
        place(part0[:3], 0),
        place(part0[3].T, 1),
        place(part1, 2),
        place(part2.T, 3),
    )


def solution(mesh):
    fused = mesh.shape["dp"] == Z_DEV * Y_DEV and mesh.shape["tensor"] == X_DEV * C_DEV
    return jax.shard_map(
        fused_step if fused else plain_step,
        mesh=mesh,
        in_specs=(
            P("dp", None),
            P("dp"),
            P(),
            P(None, None, ("dp", "tensor")),
            P(None, None, ("dp", "tensor")),
            P(None, None, "dp", "tensor"),
            P(None, "tensor", "dp"),
            P(None, "dp", "tensor"),
            P(None, "tensor", "dp"),
            P("dp", None),
        ),
        out_specs=(
            P("dp", None),
            P("dp", None),
            P(None, None, ("dp", "tensor")),
            P(None, None, ("dp", "tensor")),
            P(None, None, "dp", "tensor"),
            P(None, "tensor", "dp"),
            P(None, "dp", "tensor"),
            P(None, "tensor", "dp"),
        ),
        check_vma=False,
    )
```

```python
import jax
import jax.numpy as jnp
from jax import lax
from jax.experimental import pallas as pl
from jax.experimental.pallas import tpu as pltpu
from jax.sharding import PartitionSpec as P

D = 768
HEAD_DIM = 64
FF = 3072
NSRC = 4
EPS = 1e-05
MASKED = -1e30
F32 = jnp.float32
BF16 = jnp.bfloat16
VMEM_LIMIT = 60 * 1024 * 1024


def dot_nn(a, b):
    return lax.dot_general(a, b, (((1,), (0,)), ((), ())), preferred_element_type=F32)


def dot_nt(a, b):
    return lax.dot_general(a, b, (((1,), (1,)), ((), ())), preferred_element_type=F32)


def norm_parts(v):
    center = jnp.mean(v, -1, keepdims=True)
    centered = v - center
    r = lax.rsqrt(jnp.mean(centered * centered, -1, keepdims=True) + EPS)
    return centered * r, r


def head_mask(shape, h):
    lane = lax.broadcasted_iota(jnp.int32, shape, 1)
    return (lane >= h * HEAD_DIM) & (lane < (h + 1) * HEAD_DIM)


def blocks(total, size):
    return [slice(i * size, (i + 1) * size) for i in range(total // size)]


def attention_forward(
    len_ref, x_ref, g_ref, rows_ref, bqv_ref,
    q_ref, v_ref, kt_ref, p_ref, o_ref, a1t_ref, h1_ref, a2_ref, a2t_ref,
    a1_ref, k_ref, vt_ref, ot_ref, attn_ref,
):
    t = pl.program_id(0)
    n = x_ref.shape[0]
    width = g_ref.shape[-1]
    heads = width // HEAD_DIM
    step = 256
    length = len_ref[0]

    @pl.when(t == 0)
    def _():
        @pl.loop(0, n // step)
        def _(b):
            rows = pl.ds(pl.multiple_of(b * step, step), step)
            xhat, _ = norm_parts(x_ref[rows, :].astype(F32))
            a1 = xhat * rows_ref[0:1, :] + rows_ref[2:3, :]
            a1_ref[rows, :] = a1.astype(BF16)
            a1t_ref[:, rows] = a1.astype(BF16).T
            attn_ref[rows, :] = x_ref[rows, :].astype(F32) + rows_ref[5:6, :]

    @pl.loop(0, n // step)
    def _(b):
        rows = pl.ds(pl.multiple_of(b * step, step), step)
        a1 = a1_ref[rows, :]
        q = (dot_nn(a1, g_ref[0, 0]) + bqv_ref[0, 0:1, :]).astype(BF16)
        q_ref[0, rows, :] = q * jnp.asarray(HEAD_DIM ** -0.5, BF16)
        k = dot_nn(a1, g_ref[0, 1]).astype(BF16)
        k_ref[rows, :] = k
        kt_ref[0, :, rows] = k.T
        v = (dot_nn(a1, g_ref[0, 2]) + bqv_ref[0, 1:2, :]).astype(BF16)
        v_ref[0, rows, :] = v
        vt_ref[:, rows] = v.T

    for h in range(heads):
        k = k_ref[...]
        k = jnp.where(head_mask(k.shape, h), k, jnp.zeros_like(k))
        for b in range(n // step):
            first, last = b * step, (b + 1) * step
            q = q_ref[0, first:last, :]
            key = lax.broadcasted_iota(jnp.int32, (last, step), 0)
            query = lax.broadcasted_iota(jnp.int32, (step, step), 1) + first
            s = dot_nt(k[:last], q)
            near = jnp.where(
                (key[first:] <= query) & (key[first:] < length), s[first:], MASKED
            )
            if b:
                far = jnp.where(key[:first] < length, s[:first], MASKED)
                top = jnp.maximum(
                    jnp.max(far, 0, keepdims=True), jnp.max(near, 0, keepdims=True)
                )
                e_far = jnp.exp(far - top)
                e_near = jnp.exp(near - top)
                total = jnp.sum(e_far, 0, keepdims=True) + jnp.sum(e_near, 0, keepdims=True)
                scale = 1.0 / total
                p_ref[0, h, :first, first:last] = (e_far * scale).astype(BF16)
            else:
                top = jnp.max(near, 0, keepdims=True)
                e_near = jnp.exp(near - top)
                scale = 1.0 / jnp.sum(e_near, 0, keepdims=True)
            p_ref[0, h, first:last, first:last] = (e_near * scale).astype(BF16)
            ot_ref[h * HEAD_DIM : (h + 1) * HEAD_DIM, first:last] = dot_nn(
                vt_ref[h * HEAD_DIM : (h + 1) * HEAD_DIM, :last],
                p_ref[0, h, :last, first:last],
            ).astype(BF16)

    @pl.loop(0, n // step)
    def _(b):
        rows = pl.ds(pl.multiple_of(b * step, step), step)
        o = ot_ref[:, rows].T
        o_ref[0, rows, :] = o
        attn_ref[rows, :] += dot_nt(o, g_ref[0, 3])

    @pl.when(t == pl.num_programs(0) - 1)
    def _():
        @pl.loop(0, n // step)
        def _(b):
            rows = pl.ds(pl.multiple_of(b * step, step), step)
            h1 = attn_ref[rows, :]
            h1_ref[rows, :] = h1
            xhat, _ = norm_parts(h1)
            a2 = (xhat * rows_ref[1:2, :] + rows_ref[6:7, :]).astype(BF16)
            a2_ref[rows, :] = a2
            a2t_ref[:, rows] = a2.T


SQRT_2_PI = 0.7978845608028654


def feed_forward_both(
    len_ref, c_ref, a2_ref, a2t_ref, h1_ref, w1_ref, w2_ref, rows_ref,
    out_ref, d1_ref, d2_ref, dh1_ref, gb_ref, gbt_ref, sums_ref,
    gf_ref, gft_ref, feed_ref, da2_ref, h_ref, df_ref,
):
    t = pl.program_id(0)
    n = c_ref.shape[0]
    step = 256
    length = len_ref[0]

    @pl.when(t == 0)
    def _():
        sums_ref[...] = jnp.zeros_like(sums_ref)

        @pl.loop(0, n // step)
        def _(b):
            rows = pl.ds(pl.multiple_of(b * step, step), step)
            place = b * step + lax.broadcasted_iota(jnp.int32, (step, 1), 0)
            live = (place < length).astype(F32)
            g = (c_ref[rows, :].astype(F32) * live).astype(BF16)
            gf_ref[rows, :] = g
            gft_ref[:, rows] = g.T
            sums_ref[7:8, :] += jnp.sum(g.astype(F32), 0, keepdims=True)

    bias = rows_ref[pl.ds(8 + t, 1), :]

    @pl.loop(0, n // step)
    def _(b):
        rows = pl.ds(pl.multiple_of(b * step, step), step)
        f = dot_nn(a2_ref[rows, :], w1_ref[0]) + bias
        dh = dot_nn(gf_ref[rows, :], w2_ref[0])
        f2 = f * f
        th = jnp.tanh(f * (SQRT_2_PI + (SQRT_2_PI * 0.044715) * f2))
        half = 0.5 + 0.5 * th
        h = (f * half).astype(BF16)
        slope = half + f * (0.5 - 0.5 * th * th) * (
            SQRT_2_PI + (3 * SQRT_2_PI * 0.044715) * f2
        )
        df = (dh * slope).astype(BF16)
        h_ref[rows, :] = h
        df_ref[rows, :] = df
        sums_ref[pl.ds(8 + t, 1), :] += jnp.sum(df.astype(F32), 0, keepdims=True)
        feed = dot_nt(h, w2_ref[0])
        da2 = dot_nt(df, w1_ref[0])

        @pl.when(t == 0)
        def _():
            feed_ref[rows, :] = feed
            da2_ref[rows, :] = da2

        @pl.when(t > 0)
        def _():
            feed_ref[rows, :] += feed
            da2_ref[rows, :] += da2

    @pl.loop(0, D // step)
    def _(b):
        rows = pl.ds(pl.multiple_of(b * step, step), step)
        d1_ref[0, rows, :] = dot_nn(a2t_ref[rows, :], df_ref[...]).astype(BF16)
        d2_ref[0, rows, :] = dot_nn(gft_ref[rows, :], h_ref[...]).astype(BF16)

    @pl.when(t == pl.num_programs(0) - 1)
    def _():
        @pl.loop(0, n // step)
        def _(b):
            rows = pl.ds(pl.multiple_of(b * step, step), step)
            place = b * step + lax.broadcasted_iota(jnp.int32, (step, 1), 0)
            live = (place < length).astype(F32)
            h1 = h1_ref[rows, :]
            out_ref[rows, :] = (live * (h1 + (feed_ref[rows, :] + rows_ref[7:8, :]))).astype(BF16)
            xhat, r = norm_parts(h1)
            da2 = da2_ref[rows, :]
            sums_ref[1:2, :] += jnp.sum(da2 * xhat, 0, keepdims=True)
            sums_ref[6:7, :] += jnp.sum(da2, 0, keepdims=True)
            dg = da2 * rows_ref[1:2, :]
            dv = r * (
                dg
                - jnp.mean(dg, -1, keepdims=True)
                - xhat * jnp.mean(dg * xhat, -1, keepdims=True)
            )
            dh1 = live * c_ref[rows, :].astype(F32) + dv
            dh1_ref[rows, :] = dh1
            gb = dh1.astype(BF16)
            gb_ref[rows, :] = gb
            gbt_ref[:, rows] = gb.T
            sums_ref[5:6, :] += jnp.sum(gb.astype(F32), 0, keepdims=True)


def attention_backward(
    x_ref, g_ref, rows_ref, dh1_ref, gb_ref, gbt_ref, q_ref, v_ref, kt_ref, p_ref,
    o_ref, a1t_ref,
    d0_ref, xg_ref, sums_ref, bqv_ref,
    do_ref, delta_ref, dqt_ref, dq_ref, dk_ref, dv_ref, da1_ref,
):
    t = pl.program_id(0)
    n = x_ref.shape[0]
    width = g_ref.shape[-1]
    heads = width // HEAD_DIM
    step = 256
    pick = (
        lax.broadcasted_iota(jnp.int32, (16, width), 1) // HEAD_DIM
        == lax.broadcasted_iota(jnp.int32, (16, width), 0)
    ).astype(BF16)

    @pl.loop(0, n // step)
    def _(b):
        rows = pl.ds(pl.multiple_of(b * step, step), step)
        do = dot_nn(gb_ref[rows, :], g_ref[0, 3]).astype(BF16)
        do_ref[rows, :] = do
        prod = do.astype(F32) * o_ref[0, rows, :].astype(F32)
        high = prod.astype(BF16)
        low = (prod - high.astype(F32)).astype(BF16)
        delta_ref[:, rows] = dot_nt(pick, high) + dot_nt(pick, low)

    dqt_ref[...] = jnp.zeros_like(dqt_ref)
    for b in range(n // step):
        first, last = b * step, (b + 1) * step
        do = do_ref[first:, :]
        q = q_ref[0, first:, :]
        v = v_ref[0, first:last, :]
        dk, dv = None, None
        for h in range(heads):
            mine = head_mask((1, width), h)
            zero = jnp.zeros((), BF16)
            p = p_ref[0, h, first:last, first:]
            dp = dot_nt(jnp.where(mine, v, zero), do)
            ds = (p.astype(F32) * (dp - delta_ref[h : h + 1, first:])).astype(BF16)
            part = dot_nn(p, jnp.where(mine, do, zero))
            dv = part if dv is None else dv + part
            part = dot_nn(ds, jnp.where(mine, q, zero))
            dk = part if dk is None else dk + part
            head = slice(h * HEAD_DIM, (h + 1) * HEAD_DIM)
            dqt_ref[head, first:] += dot_nn(kt_ref[0, head, first:last], ds)
        dk_ref[first:last, :] = dk.astype(BF16)
        dv_ref[first:last, :] = dv.astype(BF16)

    @pl.when(t == 0)
    def _():
        da1_ref[...] = jnp.zeros_like(da1_ref)

    bqv_ref[...] = jnp.zeros_like(bqv_ref)

    @pl.loop(0, n // step)
    def _(b):
        rows = pl.ds(pl.multiple_of(b * step, step), step)
        dq = (dqt_ref[:, rows] * HEAD_DIM ** -0.5).astype(BF16).T
        dk = dk_ref[rows, :]
        dv = dv_ref[rows, :]
        dq_ref[rows, :] = dq
        bqv_ref[0, 0:1, :] += jnp.sum(dq.astype(F32), 0, keepdims=True)
        bqv_ref[0, 1:2, :] += jnp.sum(dv.astype(F32), 0, keepdims=True)
        da1_ref[rows, :] += (
            dot_nt(dq, g_ref[0, 0]) + dot_nt(dk, g_ref[0, 1]) + dot_nt(dv, g_ref[0, 2])
        )

    @pl.loop(0, D // step)
    def _(b):
        rows = pl.ds(pl.multiple_of(b * step, step), step)
        a1t = a1t_ref[rows, :]
        d0_ref[0, 0, rows, :] = dot_nn(a1t, dq_ref[...]).astype(BF16)
        d0_ref[0, 1, rows, :] = dot_nn(a1t, dk_ref[...]).astype(BF16)
        d0_ref[0, 2, rows, :] = dot_nn(a1t, dv_ref[...]).astype(BF16)
        d0_ref[0, 3, rows, :] = dot_nn(gbt_ref[rows, :], o_ref[0]).astype(BF16)

    @pl.when(t == pl.num_programs(0) - 1)
    def _():
        sums_ref[...] = jnp.zeros_like(sums_ref)

        @pl.loop(0, n // step)
        def _(b):
            rows = pl.ds(pl.multiple_of(b * step, step), step)
            xhat, r = norm_parts(x_ref[rows, :].astype(F32))
            da1 = da1_ref[rows, :]
            sums_ref[0:1, :] += jnp.sum(da1 * xhat, 0, keepdims=True)
            sums_ref[1:2, :] += jnp.sum(da1, 0, keepdims=True)
            dg = da1 * rows_ref[0:1, :]
            dv = r * (
                dg
                - jnp.mean(dg, -1, keepdims=True)
                - xhat * jnp.mean(dg * xhat, -1, keepdims=True)
            )
            xg_ref[rows, :] = (dh1_ref[rows, :] + dv).astype(BF16)


def whole(*shape):
    return pl.BlockSpec(shape, lambda t: (0,) * len(shape))


def group(*shape):
    return pl.BlockSpec((1,) + shape, lambda t: (t,) + (0,) * len(shape))


def shaped(dtype, *shape):
    return jax.ShapeDtypeStruct(shape, dtype)


SMEM_WHOLE = pl.BlockSpec(memory_space=pltpu.SMEM)


def run_attention_forward(length, x, g0, rows, bqv):
    n = x.shape[0]
    groups, _, _, width = g0.shape
    heads = width // HEAD_DIM
    return pl.pallas_call(
        attention_forward,
        grid=(groups,),
        in_specs=[SMEM_WHOLE, whole(n, D), group(4, D, width), whole(16, D), group(2, width)],
        out_specs=[
            group(n, width), group(n, width), group(width, n), group(heads, n, n),
            group(n, width), whole(D, n), whole(n, D), whole(n, D), whole(D, n),
        ],
        out_shape=[
            shaped(BF16, groups, n, width), shaped(BF16, groups, n, width),
            shaped(BF16, groups, width, n), shaped(BF16, groups, heads, n, n),
            shaped(BF16, groups, n, width), shaped(BF16, D, n), shaped(F32, n, D),
            shaped(BF16, n, D), shaped(BF16, D, n),
        ],
        scratch_shapes=[
            pltpu.VMEM((n, D), BF16), pltpu.VMEM((n, width), BF16),
            pltpu.VMEM((width, n), BF16), pltpu.VMEM((width, n), BF16),
            pltpu.VMEM((n, D), F32),
        ],
        compiler_params=pltpu.CompilerParams(vmem_limit_bytes=VMEM_LIMIT),
        name="attention_forward",
    )(length, x, g0, rows, bqv)


def run_feed_forward(length, cot, a2, a2t, h1, g1, g2, rows):
    n = cot.shape[0]
    groups, _, width = g1.shape
    return pl.pallas_call(
        feed_forward_both,
        grid=(groups,),
        in_specs=[
            SMEM_WHOLE, whole(n, D), whole(n, D), whole(D, n), whole(n, D),
            group(D, width), group(D, width), whole(16, D),
        ],
        out_specs=[
            whole(n, D), group(D, width), group(D, width), whole(n, D), whole(n, D),
            whole(D, n), whole(16, D),
        ],
        out_shape=[
            shaped(BF16, n, D), shaped(BF16, groups, D, width), shaped(BF16, groups, D, width),
            shaped(F32, n, D), shaped(BF16, n, D), shaped(BF16, D, n), shaped(F32, 16, D),
        ],
        scratch_shapes=[
            pltpu.VMEM((n, D), BF16), pltpu.VMEM((D, n), BF16), pltpu.VMEM((n, D), F32),
            pltpu.VMEM((n, D), F32), pltpu.VMEM((n, width), BF16), pltpu.VMEM((n, width), BF16),
        ],
        compiler_params=pltpu.CompilerParams(vmem_limit_bytes=VMEM_LIMIT),
        name="feed_forward_both",
    )(length, cot, a2, a2t, h1, g1, g2, rows)


def run_attention_backward(x, g0, rows, dh1, gb, gbt, q, v, kt, p, o, a1t):
    n = x.shape[0]
    groups, _, _, width = g0.shape
    heads = width // HEAD_DIM
    return pl.pallas_call(
        attention_backward,
        grid=(groups,),
        in_specs=[
            whole(n, D), group(4, D, width), whole(16, D), whole(n, D), whole(n, D),
            whole(D, n), group(n, width), group(n, width), group(width, n),
            group(heads, n, n), group(n, width), whole(D, n),
        ],
        out_specs=[group(4, D, width), whole(n, D), whole(8, D), group(8, width)],
        out_shape=[
            shaped(BF16, groups, 4, D, width), shaped(BF16, n, D), shaped(F32, 8, D),
            shaped(F32, groups, 8, width),
        ],
        scratch_shapes=[
            pltpu.VMEM((n, width), BF16), pltpu.VMEM((16, n), F32), pltpu.VMEM((width, n), F32),
            pltpu.VMEM((n, width), BF16), pltpu.VMEM((n, width), BF16),
            pltpu.VMEM((n, width), BF16), pltpu.VMEM((n, D), F32),
        ],
        compiler_params=pltpu.CompilerParams(vmem_limit_bytes=VMEM_LIMIT),
        name="attention_backward",
    )(x, g0, rows, dh1, gb, gbt, q, v, kt, p, o, a1t)


Z_DEV, Y_DEV, X_DEV, C_DEV = 4, 2, 2, 2


class Place:
    def __init__(self):
        dp, self.t = lax.axis_index("dp"), lax.axis_index("tensor")
        self.dp = dp
        self.z, self.y = dp // 2, dp % 2
        self.x, self.c = self.t // 2, self.t % 2
        self.other_y = 1 - self.y
        self.zs = [
            self.z,
            self.z + 1 - 2 * (self.z % 2),
            self.z + 2 - 4 * (self.z // 2),
            3 - self.z,
        ]
        self.ts = [
            self.t,
            self.t + 1 - 2 * (self.t % 2),
            self.t + 2 - 4 * (self.t // 2),
            3 - self.t,
        ]
        self.to_z = [dict(dp=z * 2 + self.y) for z in self.zs]
        self.to_y = dict(dp=self.z * 2 + self.other_y)
        self.to_x = dict(tensor=self.ts[2])
        self.same_t = self.to_z[1:] + [dict(dp=z * 2 + self.other_y) for z in self.zs]
        self.same_dp = [dict(tensor=t) for t in self.ts[1:]]
        self.to_core = dict(tensor=self.ts[1])

    def group(self, k):
        return lax.select(
            k == 0, self.ts[0],
            lax.select(k == 1, self.ts[1], lax.select(k == 2, self.ts[2], self.ts[3])),
        )

    def greet(self, others=None):
        barrier = pltpu.get_barrier_semaphore()
        others = others or self.to_z[1:] + [self.to_y, self.to_x, self.to_core]
        for device in others:
            pl.semaphore_signal(
                barrier, inc=1, device_id=device, device_id_type=pl.DeviceIdType.MESH
            )
        pl.semaphore_wait(barrier, len(others))


class Links:
    def __init__(self, send_sem, recv_sem):
        self.send_sem, self.recv_sem = send_sem, recv_sem
        self.copies = []

    def add(self, device, src, dst):
        number = len(self.copies)
        copy = pltpu.make_async_remote_copy(
            src_ref=src,
            dst_ref=dst,
            send_sem=self.send_sem.at[number],
            recv_sem=self.recv_sem.at[number],
            device_id=device,
            device_id_type=pl.DeviceIdType.MESH,
        )
        self.copies.append(copy)
        return copy

    def sent(self, *apart):
        for copy in self.copies:
            if all(copy is not other for other in apart):
                copy.wait_send()


def flat(copies):
    for item in copies:
        if isinstance(item, list):
            yield from flat(item)
        else:
            yield item


def start(*copies):
    for copy in flat(copies):
        copy.start()


def recv(*copies):
    for copy in flat(copies):
        copy.wait_recv()


class Gather:
    def __init__(self, links, place, own, full, order, single=True, last=True):
        every = slice(None)
        y, other = place.y, place.other_y

        def same(device, k, yy, to):
            return links.add(device, full(k, every, yy), full(to, every, yy))

        def along_z(k, yy, block):
            here, passed = full(k, place.z, yy), full(k, place.zs[2], yy)
            return [
                links.add(place.to_z[1], block, here),
                links.add(place.to_z[2], block, here),
                links.add(place.to_z[1], passed, passed),
            ]

        self.z = along_z(0, y, own)
        if order == X_Z_Y:
            self.first = [links.add(place.to_x, own, full(2, place.z, y))]
            self.far = along_z(2, y, full(2, place.z, y))
            blocks = [(0, y), (2, y), (0, other), (2, other)]
        else:
            blocks = [(0, y), (0, other), (2, y), (2, other)]
        if order == Y_Z_X:
            self.first = [links.add(place.to_y, own, full(0, place.z, y))]
            self.far = along_z(0, other, full(0, place.z, other))
        if order == Z_Y_X and single:
            self.first = [same(place.to_y, 0, y, 0)]
        if order == Z_Y_X and not single:
            self.first = [links.add(place.to_y, own, full(0, place.z, y))]
            for k in range(1, 4):
                block = full(0, place.zs[k], y)
                self.first.append(links.add(place.to_y, block, block))
        if not last:
            blocks = blocks[:-1]
        self.second = [
            same(place.to_y, k, yy, k) if order == X_Z_Y else same(place.to_x, k, yy, 2)
            for k, yy in blocks[:2][: 2 if last else 1]
        ]
        self.core = [same(place.to_core, k, yy, k + 1) for k, yy in blocks]


Z_Y_X, Y_Z_X, X_Z_Y = range(3)


def fused_forward(
    tie_ref, len_ref, tokens_ref, gains_ref, bias_ref, in_ref, out_ref, expand_ref,
    project_ref,
    gq_ref, gw_ref, flat1_ref, flat2_ref, rows_ref,
    q_ref, v_ref, kt_ref, p_ref, scale_ref, o_ref, a1t_out, h1_out, a2_out, a2t_out,
    own0_ref, ownw_ref, own1_ref, own2_ref, square_ref, vec_ref,
    all0_ref, allw_ref, w1_ref, w2_ref, vecs_ref, bqv_ref, x_ref, a1_ref, k_ref, qa_ref, vt_ref, ot_ref, a1t_ref, h1_ref, a2_ref, a2t_ref,
    send_sem, recv_sem, local_sem, flush_sem, row_sem,
):
    t = pl.program_id(0)
    n, _ = x_ref.shape
    width = allw_ref.shape[-1]
    heads = width // HEAD_DIM
    step = 256
    place = Place()
    length = len_ref[place.t]
    links = Links(send_sem, recv_sem)
    z, y, x, c = place.z, place.y, place.x, place.c
    mine_there = vecs_ref.at[z, y, x, c]
    column = vecs_ref.at[:, :, x, c]
    vec_one = [links.add(device, vec_ref, mine_there) for device in place.same_t]
    vec_two = [links.add(device, column, column) for device in place.same_dp]
    seg0 = Gather(
        links, place, own0_ref, lambda k, z, y: all0_ref.at[k, z, y], Z_Y_X, single=False
    )
    segw = Gather(links, place, ownw_ref, lambda k, z, y: allw_ref.at[k, z, y], Z_Y_X)
    seg1 = Gather(
        links, place, own1_ref, lambda k, z, y: w1_ref.at[k, z, y], Y_Z_X, last=False
    )
    seg2 = Gather(
        links, place, own2_ref, lambda k, z, y: w2_ref.at[k, z, y], X_Z_Y, last=False
    )
    flush = [
        [
            pltpu.make_async_copy(ref.at[k], flat.at[k], flush_sem.at[i, k])
            for k in range(4)
        ]
        for i, (ref, flat) in enumerate([(w1_ref, flat1_ref), (w2_ref, flat2_ref)])
    ]
    put_a1t = pltpu.make_async_copy(a1t_ref, a1t_out, local_sem.at[0])
    put_a2t = pltpu.make_async_copy(a2t_ref, a2t_out, local_sem.at[1])
    puts = []
    for i in range(n // step):
        rows = pl.ds(i * step, step)
        puts.append([
            pltpu.make_async_copy(h1_ref.at[rows], h1_out.at[rows], row_sem.at[0, i]),
            pltpu.make_async_copy(a2_ref.at[rows], a2_out.at[rows], row_sem.at[1, i]),
        ])
    fetch = pltpu.make_async_copy(tokens_ref.at[place.t], x_ref, local_sem.at[2])

    def relay_z(copies):
        recv(copies[1])
        start(copies[2])

    def pass_own(seg):
        recv(seg.z[0], seg.z[2])
        if seg is segw:
            start(seg.first)
        start(seg.second[0], seg.core[0])

    def pass_first(seg):
        recv(seg.first)
        if seg is segw:
            start(seg.second[1], seg.core[1])
        else:
            start(seg.far[1], seg.far[0])

    def pass_far(seg):
        recv(seg.far[0], seg.far[2])
        start(seg.core[1])

    def pass_core(seg, i):
        recv(seg.second[i])
        start(seg.core[2 + i])

    plan = [
        (0, 0, lambda: (pass_own(segw), pass_first(seg1), relay_z(seg2.z), pass_first(seg2))),
        (0, 3, lambda: (pass_first(segw), relay_z(seg1.z), pass_core(seg0, 0))),
        (1, 0, lambda: recv(seg0.core[:2])),
        (1, 1, lambda: relay_z(seg1.far)),
        (1, 3, lambda: pass_core(seg0, 1)),
        (1, 4, lambda: (recv(segw.core[:2]), pass_core(segw, 0), pass_own(seg2))),
        (2, 1, lambda: relay_z(seg2.far)),
        (2, 2, lambda: pass_core(segw, 1)),
        (2, 3, lambda: pass_own(seg1)),
        (3, 0, lambda: (recv(seg0.core[2:]), pass_far(seg1), flush[0][0].start())),
        (3, 2, lambda: (pass_far(seg2), pass_core(seg2, 0), flush[1][0].start())),
        (3, 3, lambda: flush[1][2].start()),
        (3, 4, lambda: recv(segw.core[2:])),
    ]

    def serve(point):
        for step, where, act in plan:
            if where == point:
                pl.when(t == step)(lambda act=act: (act(), None)[1])

    @pl.when(t == 0)
    def _():
        s0, s1, s2, s3 = tie_ref[0], tie_ref[1], tie_ref[2], tie_ref[3]
        fetch.start()
        square_ref[...] = jnp.zeros_like(square_ref)
        gain = gains_ref.shape[-1]
        square_ref[0:1, :gain] = gains_ref[s0].astype(F32)[0:1]
        square_ref[1:2, :gain] = gains_ref[s2].astype(F32)[1:2]
        kinds = [s0, s0, s0, s1, s2, s3, s2, s2, s2, s2]
        for i, source in enumerate(kinds):
            wide = bias_ref[i].astype(F32)
            here = lax.broadcasted_iota(jnp.int32, wide.shape, 0) == source
            square_ref[2 + i : 3 + i, :gain] = jnp.sum(
                jnp.where(here, wide, 0.0), 0, keepdims=True
            )
        vec_ref[...] = square_ref[...].T[:gain]
        for j in range(3):
            own0_ref[:, j * width : (j + 1) * width] = in_ref[s0, j]
        place.greet(place.same_t + place.same_dp)
        start(vec_one, seg0.z[1], seg0.z[0], seg0.first[0])
        vecs_ref[z, y, x, c] = vec_ref[...]
        ones = lax.broadcasted_iota(jnp.int32, (vt_ref.shape[1] - HEAD_DIM, n), 0) == 0
        for h in range(heads):
            vt_ref[h, HEAD_DIM:, :] = ones.astype(BF16)
        all0_ref[0, z, y] = own0_ref[...]
        ownw_ref[...] = out_ref[s1].T
        allw_ref[0, z, y] = ownw_ref[...]
        own1_ref[...] = expand_ref[s2]
        own2_ref[...] = project_ref[s3]
        w1_ref[0, z, y] = own1_ref[...]
        w2_ref[0, z, y] = own2_ref[...]
        recv(vec_one)
        start(vec_two)
        relay_z(seg0.z)
        start(seg0.first[2])
        recv(seg0.z[0])
        start(seg0.first[1], segw.z[1], segw.z[0], seg2.z[1])
        recv(vec_two)
        start(seg2.first)
        vecs = vecs_ref[...].reshape(D, vecs_ref.shape[-1]).T[:16]
        rows_ref[...] = vecs
        recv(seg0.z[2])
        start(seg0.first[3], seg1.first, seg0.second[0], seg0.core[0])
        for k in range(4):
            part = slice(k * width, (k + 1) * width)
            bqv_ref[k, 0:1, :width] = vecs[3:4, part]
            bqv_ref[k, 0:1, width : 2 * width] = jnp.zeros((1, width), F32)
            bqv_ref[k, 0:1, 2 * width :] = vecs[4:5, part]
        fetch.wait()

        @pl.loop(0, n // step)
        def _(b):
            rows = pl.ds(pl.multiple_of(b * step, step), step)
            wide = x_ref[rows, :].astype(F32)
            xhat, _ = norm_parts(wide)
            a1 = (xhat * rows_ref[0:1, :] + rows_ref[2:3, :]).astype(BF16)
            a1_ref[rows, :] = a1
            a1t_ref[:, rows] = a1.T
            h1_ref[rows, :] = wide + rows_ref[5:6, :]

        put_a1t.start()
        relay_z(segw.z)
        start(seg2.z[0], seg1.z[1], seg1.z[0])
        recv(seg0.first)
        start(seg0.second[1], seg0.core[1])

    serve(0)
    gq = all0_ref[t].reshape(D, 3 * width)
    gq_ref[0] = gq
    mine = place.group(t)
    qkv = dot_nn(a1_ref[...], gq) + bqv_ref[mine, 0:1, :]
    q = qkv[:, :width].astype(BF16) * jnp.asarray(HEAD_DIM ** -0.5, BF16)
    k = qkv[:, width : 2 * width].astype(BF16)
    v = qkv[:, 2 * width :].astype(BF16)
    q_ref[0] = q
    kt_ref[0] = k.T
    v_ref[0] = v
    vt = v.T
    for h in range(heads):
        vt_ref[h, :HEAD_DIM, :] = vt[h * HEAD_DIM : (h + 1) * HEAD_DIM]
    spare = k_ref.shape[1] - width
    dead = lax.broadcasted_iota(jnp.int32, (n, spare), 0) >= length
    first_column = lax.broadcasted_iota(jnp.int32, (n, spare), 1) == 0
    k_ref[:, :width] = k
    k_ref[:, width:] = jnp.where(first_column & dead, MASKED, 0.0).astype(BF16)
    qa_ref[:, :width] = q
    qa_ref[:, width:] = jnp.where(first_column, 1.0, 0.0).astype(BF16)

    serve(1)
    def scores(h, b):
        first, last = b * step, (b + 1) * step
        q = qa_ref[first:last, :]
        lane = lax.broadcasted_iota(jnp.int32, (1, q.shape[1]), 1)
        keep = head_mask((1, q.shape[1]), h) | (lane >= width)
        return dot_nt(k_ref[:last, :], jnp.where(keep, q, jnp.zeros((), BF16)))

    def attend(h, b, s):
        first, last = b * step, (b + 1) * step
        key = lax.broadcasted_iota(jnp.int32, (step, step), 0)
        query = lax.broadcasted_iota(jnp.int32, (step, step), 1)
        near = jnp.where(key <= query, s[first:], MASKED)
        top = jnp.max(near, 0, keepdims=True)
        if b:
            far = s[:first]
            top = jnp.maximum(top, jnp.max(far, 0, keepdims=True))
        e_near = jnp.exp((near - top).astype(BF16))
        p_ref[0, h, first:last, first:last] = e_near
        o = dot_nn(vt_ref[h, :, first:last], e_near)
        if b:
            e_far = jnp.exp((far - top).astype(BF16))
            p_ref[0, h, :first, first:last] = e_far
            o += dot_nn(vt_ref[h, :, :first], e_far)
        scale = 1.0 / o[HEAD_DIM : HEAD_DIM + 1]
        scale_ref[0, h : h + 1, first:last] = scale
        ot_ref[h * HEAD_DIM : (h + 1) * HEAD_DIM, first:last] = (
            o[:HEAD_DIM] * scale
        ).astype(BF16)

    scale_ref[0, heads:, :] = jnp.zeros((scale_ref.shape[1] - heads, n), F32)
    for h in range(heads):
        s = scores(h, 0)
        for b in range(n // step):
            ahead = scores(h, b + 1) if b + 1 < n // step else None
            attend(h, b, s)
            s = ahead
        serve(2 + h)

    gw_ref[0] = allw_ref[t].reshape(gw_ref.shape[1:])
    o = ot_ref[...].T
    o_ref[0] = o
    h1_ref[...] += dot_nt(o, gw_ref[0])

    @pl.when(t == 3)
    def _():
        for i, rows in enumerate(blocks(n, step)):
            xhat, _ = norm_parts(h1_ref[rows, :])
            a2 = (xhat * rows_ref[1:2, :] + rows_ref[6:7, :]).astype(BF16)
            a2_ref[rows, :] = a2
            a2t_ref[:, rows] = a2.T
            for put in puts[i]:
                put.start()
        put_a2t.start()
        pass_core(seg1, 0)
        flush[0][2].start()
        recv(seg2.core)
        flush[1][1].start()
        flush[1][3].start()
        recv(seg1.core)
        flush[0][1].start()
        flush[0][3].start()
        links.sent()
        for copies in flush + puts + [[put_a1t, put_a2t]]:
            for copy in copies:
                copy.wait()


N_GATHER = 10 + 13 + 10 + 11 + 11
VMEM_WHOLE = pl.BlockSpec(memory_space=pltpu.VMEM)
ANY_WHOLE = pl.BlockSpec(memory_space=pl.ANY)


def run_fused_forward(tie, lengths, tokens, gains, biases, w_in, w_out, w_expand, w_project):
    groups, n, _ = tokens.shape
    depth, width = w_in.shape[-2:]
    heads = width // HEAD_DIM
    hidden = w_expand.shape[-1]
    w_project = w_project.transpose(0, 2, 1)
    biases = biases.transpose(1, 0, 2)
    own = gains.shape[-1]
    return pl.pallas_call(
        fused_forward,
        grid=(groups,),
        in_specs=[SMEM_WHOLE, SMEM_WHOLE, ANY_WHOLE] + [VMEM_WHOLE] * 6,
        out_specs=[
            group(D, 3 * width), group(D, width), ANY_WHOLE, ANY_WHOLE, VMEM_WHOLE,
            group(n, width), group(n, width), group(width, n), group(heads, n, n),
            group(8, n), group(n, width), ANY_WHOLE, ANY_WHOLE, ANY_WHOLE, ANY_WHOLE,
        ],
        out_shape=[
            shaped(BF16, groups, D, 3 * width), shaped(BF16, groups, D, width),
            shaped(BF16, groups, Z_DEV, Y_DEV, depth, hidden),
            shaped(BF16, groups, Z_DEV, Y_DEV, depth, hidden),
            shaped(F32, 16, D),
            shaped(BF16, groups, n, width), shaped(BF16, groups, n, width),
            shaped(BF16, groups, width, n), shaped(BF16, groups, heads, n, n),
            shaped(F32, groups, 8, n), shaped(BF16, groups, n, width), shaped(BF16, D, n), shaped(F32, n, D),
            shaped(BF16, n, D), shaped(BF16, D, n),
        ],
        scratch_shapes=[
            pltpu.VMEM((depth, 3 * width), BF16), pltpu.VMEM((depth, width), BF16),
            pltpu.VMEM((depth, hidden), BF16), pltpu.VMEM((depth, hidden), BF16),
            pltpu.VMEM((128, 128), F32), pltpu.VMEM((own, 128), F32),
            pltpu.VMEM((groups, Z_DEV, Y_DEV, depth, 3 * width), BF16),
            pltpu.VMEM((groups, Z_DEV, Y_DEV, depth, width), BF16),
            pltpu.VMEM((groups, Z_DEV, Y_DEV, depth, hidden), BF16),
            pltpu.VMEM((groups, Z_DEV, Y_DEV, depth, hidden), BF16),
            pltpu.VMEM((Z_DEV, Y_DEV, X_DEV, C_DEV, own, 128), F32),
            pltpu.VMEM((groups, 8, 3 * width), F32),
            pltpu.VMEM((n, D), BF16), pltpu.VMEM((n, D), BF16), pltpu.VMEM((n, 256), BF16),
            pltpu.VMEM((n, 256), BF16), pltpu.VMEM((heads, HEAD_DIM + 16, n), BF16),
            pltpu.VMEM((width, n), BF16),
            pltpu.VMEM((D, n), BF16), pltpu.VMEM((n, D), F32), pltpu.VMEM((n, D), BF16),
            pltpu.VMEM((D, n), BF16),
            pltpu.SemaphoreType.DMA((N_GATHER,)), pltpu.SemaphoreType.DMA((N_GATHER,)),
            pltpu.SemaphoreType.DMA((3,)), pltpu.SemaphoreType.DMA((2, 4)),
            pltpu.SemaphoreType.DMA((2, n // 256)),
        ],
        compiler_params=pltpu.CompilerParams(
            vmem_limit_bytes=VMEM_LIMIT, collective_id=0, has_side_effects=True
        ),
        name="fused_forward",
    )(tie, lengths, tokens, gains, biases, w_in, w_out, w_expand, w_project)


class Result:
    def __init__(self, links, place, own_ref, passing_ref, out_ref, step, sem):
        count = own_ref.shape[0] // step
        self.x, self.core, self.far, self.keep, self.keep_far = [], [], [], [], []
        for i in range(count):
            rows = pl.ds(i * step, step)
            mine, theirs = out_ref.at[place.t, rows], out_ref.at[place.ts[2], rows]
            own, passing = own_ref.at[rows], passing_ref.at[rows]
            self.x.append(links.add(place.to_x, own, passing))
            self.core.append(links.add(place.to_core, own, mine))
            self.far.append(links.add(place.to_core, passing, theirs))
            self.keep.append(pltpu.make_async_copy(own, mine, sem.at[0, i]))
            self.keep_far.append(pltpu.make_async_copy(passing, theirs, sem.at[1, i]))

    def send(self, i):
        start(self.x[i], self.core[i], self.keep[i])

    def pass_on(self, i):
        recv(self.x[i])
        start(self.far[i], self.keep_far[i])

    def finish(self):
        recv(self.core, self.far)
        for copy in self.keep + self.keep_far:
            copy.wait()


def pair_order(i):
    return i + 1 - 2 * (i % 2)


def fused_feed_forward(
    len_ref, cot_ref, a2_ref, a2t_in, h1_in, far1_ref, far2_ref, rows_ref,
    out_out, fold_ref, work_out, dh1_out, gb_out, gbt_out, sums_ref,
    gf_ref, gft_ref, feed_ref, da2_ref, h_ref, df_ref, weights_ref, missing_ref,
    stage_ref, land_ref, near_ref, cross_ref, a2t_ref, h1_ref, out_ref, work_ref,
    send_sem, recv_sem, local_sem, row_sem,
):
    t = pl.program_id(0)
    n = gf_ref.shape[0]
    step = 256
    depth = stage_ref.shape[-2]
    place = Place()
    length = len_ref[place.t]
    links = Links(send_sem, recv_sem)
    y, other = place.y, place.other_y
    last = [
        links.add(place.to_x, far1_ref.at[0, :, other], missing_ref.at[0, 0]),
        links.add(place.to_y, far2_ref.at[2, :, y], missing_ref.at[1, 0]),
    ]
    last_core = [
        links.add(place.to_core, missing_ref.at[i, 0], missing_ref.at[i, 1]) for i in range(2)
    ]
    core = [
        [links.add(place.to_core, stage_ref.at[i], land_ref.at[s, i]) for i in range(2)]
        for s in range(2)
    ]
    cross = [
        links.add(place.to_y, near_ref.at[i, :, other], cross_ref.at[i]) for i in range(2)
    ]
    fetch = pltpu.make_async_copy(cot_ref.at[place.t], gf_ref, local_sem.at[0])
    gb_ref, gbt_ref, dh1_ref = gf_ref, gft_ref, da2_ref
    late = [
        pltpu.make_async_copy(a2t_in, a2t_ref, local_sem.at[5]),
        pltpu.make_async_copy(h1_in, h1_ref, local_sem.at[6]),
    ]
    puts = []
    for i in range(n // step):
        rows = pl.ds(i * step, step)
        puts.append([
            pltpu.make_async_copy(ref.at[rows], out.at[rows], row_sem.at[j, i])
            for j, (ref, out) in enumerate(
                [(out_ref, out_out), (dh1_ref, dh1_out), (gb_ref, gb_out)]
            )
        ])
    put_gbt = pltpu.make_async_copy(gbt_ref, gbt_out, local_sem.at[7])
    put_work = pltpu.make_async_copy(work_ref, work_out, local_sem.at[8])
    k = pair_order(t)
    mine = place.group(k)

    def load(step, whole, slot):
        for i, far_ref in enumerate([far1_ref, far2_ref]):
            group = far_ref.at[pair_order(step)]
            to = weights_ref.at[slot, i]
            if not whole:
                group, to = group.at[:, y], to.at[:, y]
            yield pltpu.make_async_copy(group, to, local_sem.at[1 + 2 * slot + i])

    def live_rows(b):
        at = b * step + lax.broadcasted_iota(jnp.int32, (step, 1), 0)
        return (at < length).astype(F32)

    @pl.when(t == 0)
    def _():
        fetch.start()
        for copy in load(0, True, 0):
            copy.start()
        for copy in late:
            copy.start()
        place.greet()
        start(last)
        sums_ref[...] = jnp.zeros_like(sums_ref)
        feed_ref[...] = jnp.zeros_like(feed_ref)
        da2_ref[...] = jnp.zeros_like(da2_ref)
        fetch.wait()

        @pl.loop(0, n // step)
        def _(b):
            rows = pl.ds(pl.multiple_of(b * step, step), step)
            g = (gf_ref[rows, :].astype(F32) * live_rows(b)).astype(BF16)
            gf_ref[rows, :] = g
            gft_ref[:, rows] = g.T
            sums_ref[7:8, :] += jnp.sum(g.astype(F32), 0, keepdims=True)

    for i in range(4):
        @pl.when(t == i)
        def _():
            if i == 2:
                recv(last_core)
            for copy in load(i, i < 2, i % 2):
                copy.wait()
            if i < 3:
                for copy in load(i + 1, i + 1 < 2, (i + 1) % 2):
                    copy.start()
            if i >= 2:
                for j in range(2):
                    weights_ref[i % 2, j, :, other] = missing_ref[j, 3 - i]

    bias = rows_ref[pl.ds(8 + mine, 1), :]
    w1 = weights_ref[t % 2, 0].reshape(D, -1)
    w2 = weights_ref[t % 2, 1].reshape(D, -1)
    column = jnp.zeros((1, w1.shape[1]), F32)
    for rows in blocks(n, step):
        f = dot_nn(a2_ref[rows, :], w1) + bias
        dh = dot_nn(gf_ref[rows, :], w2)
        f2 = f * f
        th = jnp.tanh(f * (SQRT_2_PI + (SQRT_2_PI * 0.044715) * f2))
        half = 0.5 + 0.5 * th
        h = (f * half).astype(BF16)
        slope = half + f * (0.5 - 0.5 * th * th) * (
            SQRT_2_PI + (3 * SQRT_2_PI * 0.044715) * f2
        )
        df = (dh * slope).astype(BF16)
        h_ref[rows, :] = h
        df_ref[rows, :] = df
        column += jnp.sum(df.astype(F32), 0, keepdims=True)
        feed_ref[rows, :] += dot_nt(h, w2)
        da2_ref[rows, :] += dot_nt(df, w1)
    sums_ref[pl.ds(8 + mine, 1), :] = column

    @pl.when(t == 1)
    def _():
        recv(last)
        start(last_core)

    @pl.when(t == 0)
    def _():
        late[0].wait()

    def weight_grad(left_ref, right_ref):
        value = dot_nn(left_ref[...], right_ref[...])
        return value.reshape(Z_DEV, Y_DEV, depth, value.shape[-1]).astype(BF16)

    grad1 = weight_grad(a2t_ref, df_ref)
    grad2 = weight_grad(gft_ref, h_ref)

    def put(ref):
        ref[0] = grad1
        ref[1] = grad2

    def reduced(ref):
        return lambda i, s, z: (
            ref[i, z].astype(F32) + land_ref[s, i, z].astype(F32)
        ).astype(BF16)

    @pl.when(t == 0)
    def _():
        put(stage_ref)
        start(core[0])

    @pl.when(t == 1)
    def _():
        put(near_ref)
        recv(core[0])

        @pl.loop(0, Z_DEV)
        def _(z):
            for i in range(2):
                near_ref[i, z] = reduced(near_ref)(i, 0, z)

        start(cross)

    @pl.when(t == 2)
    def _():
        for copy in core[0]:
            copy.wait_send()
        put(stage_ref)
        start(core[1])

    @pl.when(t == 3)
    def _():
        put(work_ref)
        late[1].wait()
        for i, rows in enumerate(blocks(n, step)):
            live = live_rows(i)
            h1 = h1_ref[rows, :]
            out_ref[rows, :] = (live * (h1 + (feed_ref[rows, :] + rows_ref[7:8, :]))).astype(BF16)
            xhat, r = norm_parts(h1)
            da2 = da2_ref[rows, :]
            sums_ref[1:2, :] += jnp.sum(da2 * xhat, 0, keepdims=True)
            sums_ref[6:7, :] += jnp.sum(da2, 0, keepdims=True)
            dg = da2 * rows_ref[1:2, :]
            dv = r * (
                dg
                - jnp.mean(dg, -1, keepdims=True)
                - xhat * jnp.mean(dg * xhat, -1, keepdims=True)
            )
            dh1 = gf_ref[rows, :].astype(F32) + dv
            dh1_ref[rows, :] = dh1
            gb = dh1.astype(BF16)
            gb_ref[rows, :] = gb
            gbt_ref[:, rows] = gb.T
            sums_ref[5:6, :] += jnp.sum(gb.astype(F32), 0, keepdims=True)
            for copy in puts[i]:
                copy.start()
        put_gbt.start()
        recv(core[1])

        @pl.loop(0, Z_DEV)
        def _(z):
            for i in range(2):
                work_ref[i, z] = reduced(work_ref)(i, 1, z)

        put_work.start()
        recv(cross)

        @pl.loop(0, Z_DEV)
        def _(z):
            for i in range(2):
                fold_ref[i, z] = (
                    near_ref[i, z, y].astype(F32) + cross_ref[i, z].astype(F32)
                ).astype(BF16)

        links.sent(*core[0])
        for copies in puts + [[put_gbt, put_work]]:
            for copy in copies:
                copy.wait()


def run_fused_feed_forward(lengths, cot, a2, a2t, h1, g1, g2, rows):
    n = cot.shape[1]
    groups, _, _, depth, hidden = g1.shape
    both = (2, Z_DEV, Y_DEV, depth, hidden)
    fold = (2, Z_DEV, depth, hidden)
    return pl.pallas_call(
        fused_feed_forward,
        grid=(groups,),
        in_specs=[SMEM_WHOLE, ANY_WHOLE, VMEM_WHOLE] + [ANY_WHOLE] * 4 + [VMEM_WHOLE],
        out_specs=[ANY_WHOLE, VMEM_WHOLE] + [ANY_WHOLE] * 4 + [VMEM_WHOLE],
        out_shape=[
            shaped(BF16, n, D), shaped(BF16, *fold), shaped(BF16, *both), shaped(F32, n, D),
            shaped(BF16, n, D), shaped(BF16, D, n), shaped(F32, 16, D),
        ],
        scratch_shapes=[
            pltpu.VMEM((n, D), BF16), pltpu.VMEM((D, n), BF16), pltpu.VMEM((n, D), F32),
            pltpu.VMEM((n, D), F32), pltpu.VMEM((n, hidden), BF16), pltpu.VMEM((n, hidden), BF16),
            pltpu.VMEM((2,) + both, BF16),
            pltpu.VMEM((2,) + fold, BF16), pltpu.VMEM(both, BF16), pltpu.VMEM((2,) + both, BF16),
            pltpu.VMEM(both, BF16), pltpu.VMEM(fold, BF16),
            pltpu.VMEM((D, n), BF16), pltpu.VMEM((n, D), F32), pltpu.VMEM((n, D), BF16),
            pltpu.VMEM(both, BF16),
            pltpu.SemaphoreType.DMA((10,)), pltpu.SemaphoreType.DMA((10,)),
            pltpu.SemaphoreType.DMA((9,)), pltpu.SemaphoreType.DMA((3, n // 256)),
        ],
        compiler_params=pltpu.CompilerParams(
            vmem_limit_bytes=VMEM_LIMIT, collective_id=1, has_side_effects=True
        ),
        name="fused_feed_forward",
    )(lengths, cot, a2, a2t, h1, g1, g2, rows)
class Reduce:
    def __init__(
        self, links, place, work, acc, cross_ref, far_ref, mid_ref, last_ref, side_ref,
        slots=(0, 1),
    ):
        self.place, self.work, self.acc = place, work, acc
        self.cross_ref, self.far_ref, self.mid_ref = cross_ref, far_ref, mid_ref
        self.last_ref, self.side_ref = last_ref, side_ref
        zs = place.zs
        self.y = {
            s: [
                links.add(place.to_y, work(s, zs[j], place.other_y), cross_ref.at[s, zs[j]])
                for j in (1, 3, 2, 0)
            ]
            for s in slots
        }
        self.z = [
            [
                links.add(place.to_z[1], acc(s, zs[1]), far_ref.at[s, 0]),
                links.add(place.to_z[1], acc(s, zs[3]), far_ref.at[s, 1]),
                links.add(place.to_z[2], mid_ref.at[s, 1], far_ref.at[s, 2]),
            ]
            for s in range(2)
        ]
        self.x = links.add(place.to_x, last_ref, side_ref)

    def fold_y(self, s, half):
        for i, j in [(0, 1), (1, 3), (2, 2), (3, 0)][2 * half : 2 * half + 2]:
            z = self.place.zs[j]
            recv(self.y[s][i])
            value = self.work(s, z, self.place.y)[...].astype(F32)
            self.acc(s, z)[...] = (value + self.cross_ref[s, z].astype(F32)).astype(BF16)
            if i < 2:
                start(self.z[s][i])

    def fold_z(self, s):
        recv(self.z[s][:2])
        for i in (1, 0):
            value = self.acc(s, self.place.zs[2 * i])[...].astype(F32)
            self.mid_ref[s, i] = (value + self.far_ref[s, i].astype(F32)).astype(BF16)
            if i:
                start(self.z[s][2])

    def own(self, s):
        recv(self.z[s][2])
        return self.mid_ref[s, 0].astype(F32) + self.far_ref[s, 2].astype(F32)

    def send_x(self):
        self.last_ref[...] = self.own(1).astype(BF16)
        start(self.x)

    def total(self):
        value = self.own(0)
        recv(self.x)
        return value + self.side_ref[...].astype(F32)


def fused_backward(
    tokens_ref, gq_ref, gw_ref, rows_ref, dh1_ref, gb_ref, gbt_in, q_ref, v_ref, kt_ref,
    p_ref, scale_ref, o_ref, a1t_in, layer_in, fold_in, work_in, early_ref,
    out_ref, layerout_ref, part0_ref, partw_ref, part1_ref, part2_ref, total_ref,
    a1t_ref, gbt_ref, layer_ref, fold_ref, work_ref, do_ref, delta_ref, dkv_ref, dqkv_ref, da1_ref, own_ref, passing_ref, passlayer_ref, bqv_ref,
    folded_ref, cross1_ref, far1_ref, mid1_ref, last1_ref, side1_ref,
    cross2_ref, far2_ref, mid2_ref, last2_ref, side2_ref,
    stagew_ref, landw_ref, workw_ref, crossw_ref, farw_ref, midw_ref, lastw_ref, sidew_ref,
    stage0_ref, land0_ref, work0_ref, cross0_ref, far0_ref, mid0_ref, last0_ref, side0_ref,
    sums_ref, sumland_ref,
    send_sem, recv_sem, local_sem, result_sem,
):
    t = pl.program_id(0)
    n = own_ref.shape[0]
    width = gw_ref.shape[-1]
    depth = part0_ref.shape[0]
    heads = width // HEAD_DIM
    step = n // 4
    place = Place()
    y = place.y
    links = Links(send_sem, recv_sem)
    k, i = group_and_block(t)
    mine = place.group(k)
    now = k % 2
    out = Result(links, place, own_ref, passing_ref, out_ref, step, result_sem.at[0])
    layer = Result(links, place, layer_ref, passlayer_ref, layerout_ref, step, result_sem.at[1])
    fetch = pltpu.make_async_copy(tokens_ref.at[place.t], own_ref, local_sem.at[0])
    fetch_layer, fetch_work, fetch_fold, fetch_gbt, fetch_a1t = [
        pltpu.make_async_copy(there, here, local_sem.at[1 + j])
        for j, (there, here) in enumerate([
            (layer_in, layer_ref), (work_in, work_ref), (fold_in, fold_ref),
            (gbt_in, gbt_ref), (a1t_in, a1t_ref),
        ])
    ]
    corew = [links.add(place.to_core, stagew_ref, landw_ref.at[i]) for i in range(2)]
    core0 = [links.add(place.to_core, stage0_ref, land0_ref.at[i]) for i in range(2)]
    def half_done(i, *landing):
        return Reduce(
            links, place, lambda s, z, y: work_ref.at[i, z, y],
            lambda s, z: folded_ref.at[i, z] if s else fold_ref.at[i, z],
            *landing, slots=(1,),
        )

    seg1 = half_done(0, cross1_ref, far1_ref, mid1_ref, last1_ref, side1_ref)
    seg2 = half_done(1, cross2_ref, far2_ref, mid2_ref, last2_ref, side2_ref)
    segw = Reduce(
        links, place, lambda s, z, y: workw_ref.at[s, z, y],
        lambda s, z: workw_ref.at[s, z, y],
        crossw_ref, farw_ref, midw_ref, lastw_ref, sidew_ref,
    )
    seg0 = Reduce(
        links, place, lambda s, z, y: work0_ref.at[s, z, y],
        lambda s, z: work0_ref.at[s, z, y],
        cross0_ref, far0_ref, mid0_ref, last0_ref, side0_ref,
    )
    sum_core, sum_y, *sum_z, sum_x = [
        links.add(to, sums_ref.at[i], sumland_ref.at[j])
        for j, (i, to) in enumerate(
            zip([0, 1, 2, 2, 2, 3], [place.to_core, place.to_y] + place.to_z[1:] + [place.to_x])
        )
    ]

    def when(point):
        return pl.when(t == point)

    @when(0)
    def _():
        for copy in (fetch_layer, fetch_work, fetch_fold, fetch_gbt, fetch, fetch_a1t):
            copy.start()
        place.greet()
        fetch_layer.wait()
        for i in range(4):
            layer.send(i)
        fetch_work.wait()
        start(seg1.y[1], seg2.y[1])
        fetch_fold.wait()
        start(seg1.z[0][:2], seg2.z[0][:2])
        bqv_ref[...] = jnp.zeros_like(bqv_ref)
        sums_ref[0] = early_ref[...]
        da1_ref[...] = jnp.zeros_like(da1_ref)
        fetch_gbt.wait()

    def add_core():
        recv(corew[1])

        @pl.loop(0, Z_DEV)
        def _(z):
            workw_ref[1, z] = (
                workw_ref[1, z].astype(F32) + landw_ref[1, z].astype(F32)
            ).astype(BF16)

        start(segw.y[1])

    plan = [
        (2, 1, lambda: (seg1.fold_y(1, 0), seg1.fold_z(0))),
        (3, 1, lambda: layer.pass_on(0)),
        (4, 0, lambda: (seg1.fold_y(1, 1), seg2.fold_z(0))),
        (4, 1, lambda: layer.pass_on(1)),
        (5, 1, lambda: (seg1.fold_z(1), seg2.fold_y(1, 0))),
        (8, 0, lambda: (seg2.fold_y(1, 1), layer.pass_on(2))),
        (8, 1, lambda: (seg1.send_x(), segw.fold_y(0, 0), segw.fold_y(0, 1))),
        (9, 0, add_core),
        (9, 1, lambda: (seg2.fold_z(1), seg0.fold_y(0, 0), layer.pass_on(3))),
        (10, 1, lambda: segw.fold_z(0)),
        (11, 1, lambda: (seg2.send_x(), seg0.fold_y(0, 1))),
        (12, 1, lambda: (segw.fold_y(1, 0), segw.fold_y(1, 1))),
        (13, 1, lambda: (seg0.fold_z(0), out.pass_on(3))),
        (14, 1, lambda: segw.fold_z(1)),
    ]

    def serve(point):
        for at, where, act in plan:
            if where == point:
                pl.when(t == at)(lambda act=act: (act(), None)[1])

    @pl.when((t == 0) | (t == 4) | (t == 8) | (t == 9))
    def _():
        pick = (
            lax.broadcasted_iota(jnp.int32, (8, width), 1) // HEAD_DIM
            == lax.broadcasted_iota(jnp.int32, (8, width), 0)
        ).astype(BF16)

        @pl.loop(0, n // step)
        def _(i):
            rows = pl.ds(pl.multiple_of(i * step, step), step)
            columns = scale_ref[0, :, rows].T
            lane = lax.broadcasted_iota(jnp.int32, (step, width), 1)
            scale = columns[:, heads - 1 : heads]
            for h in reversed(range(heads - 1)):
                scale = jnp.where(lane < (h + 1) * HEAD_DIM, columns[:, h : h + 1], scale)
            do = (dot_nn(gb_ref[rows, :], gw_ref[0]) * scale).astype(BF16)
            do_ref[now, rows, :] = do
            product = do.astype(F32) * o_ref[0, rows, :].astype(F32)
            high = product.astype(BF16)
            low = (product - high.astype(F32)).astype(BF16)
            delta_ref[now, :, rows] = dot_nt(pick, high) + dot_nt(pick, low)

        value = dot_nn(gbt_ref[...], o_ref[0]).reshape(Z_DEV, Y_DEV, depth, width)
        for s in range(2):
            @when(8 * s)
            def _():
                if s:
                    corew[0].wait_send()
                stagew_ref[...] = value.astype(BF16)
                start(corew[s])

        @when(4)
        def _():
            recv(corew[0])
            workw_ref[0] = (value + landw_ref[0].astype(F32)).astype(BF16)
            start(segw.y[0])

        @when(9)
        def _():
            workw_ref[1] = value.astype(BF16)

    serve(0)

    for ii in reversed(range(4)):
        @pl.when(i == ii)
        def _():
            first, last = ii * step, (ii + 1) * step
            do = do_ref[now, first:last, :]
            q = q_ref[0, first:last, :]
            v = v_ref[0, :last, :]
            lane = lax.broadcasted_iota(jnp.int32, (1, width), 1)
            dk, dv, dq = None, None, []
            for h in range(heads):
                low, high = h * HEAD_DIM, (h + 1) * HEAD_DIM
                here = (lane >= low) & (lane < high)
                p = p_ref[0, h, :last, :]
                dp = dot_nt(v, jnp.where(here, do, jnp.zeros((), BF16)))
                ds = p * (dp - delta_ref[now, h : h + 1, first:last]).astype(BF16)
                part = dot_nn(p, do)
                dv = part if dv is None else jnp.where(lane < low, dv, part)
                part = dot_nn(ds, q)
                dk = part if dk is None else jnp.where(lane < low, dk, part)
                dq.append(dot_nn(kt_ref[0, low:high, :last], ds))
            if ii == 3:
                dkv_ref[now, 0] = dk
                dkv_ref[now, 1] = dv
            else:
                dkv_ref[now, 0, :last, :] += dk
                dkv_ref[now, 1, :last, :] += dv
            dk = dkv_ref[now, 0, first:last, :].astype(BF16)
            dv = dkv_ref[now, 1, first:last, :].astype(BF16)
            dq = (jnp.concatenate(dq, 0) * HEAD_DIM ** -0.5).astype(BF16).T
            dqkv_ref[now, first:last, :width] = dq
            dqkv_ref[now, first:last, width : 2 * width] = dk
            dqkv_ref[now, first:last, 2 * width :] = dv
            bqv_ref[mine, 0:1, :] += jnp.sum(dq.astype(F32), 0, keepdims=True)
            bqv_ref[mine, 1:2, :] += jnp.sum(dv.astype(F32), 0, keepdims=True)
            da1_ref[first:last, :] += dot_nt(dqkv_ref[now, first:last, :], gq_ref[0])

    serve(1)

    @pl.when((t > 8) & (t % 2 == 1))
    def _():
        rows = pl.ds(pl.multiple_of(i * step, step), step)
        xhat, r = norm_parts(own_ref[rows, :].astype(F32))
        da1 = da1_ref[rows, :]
        sums_ref[0, 0:1, :] += jnp.sum(da1 * xhat, 0, keepdims=True)
        sums_ref[0, 2:3, :] += jnp.sum(da1, 0, keepdims=True)
        dg = da1 * rows_ref[0:1, :]
        dv = r * (
            dg
            - jnp.mean(dg, -1, keepdims=True)
            - xhat * jnp.mean(dg * xhat, -1, keepdims=True)
        )
        own_ref[rows, :] = (dh1_ref[...] + dv).astype(BF16)
        for ii in range(4):
            @pl.when(i == ii)
            def _():
                out.send(ii)

    @pl.when((t == 3) | (t == 7) | (t > 13))
    def _():
        @when(3)
        def _():
            fetch.wait()
            fetch_a1t.wait()

        value = dot_nn(a1t_ref[...], dqkv_ref[now]).reshape(Z_DEV, Y_DEV, depth, 3 * width)
        for s in range(2):
            @when(3 + 11 * s)
            def _():
                if s:
                    core0[0].wait_send()
                stage0_ref[...] = value.astype(BF16)
                start(core0[s])

            @when(7 + 8 * s)
            def _():
                recv(core0[s])
                work0_ref[s] = (value + land0_ref[s].astype(F32)).astype(BF16)
                start(seg0.y[s])

    @when(15)
    def _():
        for s in range(4):
            sums_ref[0, 3:5, s * width : (s + 1) * width] = bqv_ref[s, 0:2, :]
        start(sum_core)
        segw.send_x()
        out.pass_on(2)
        recv(sum_core)
        sums_ref[1] = sums_ref[0] + sumland_ref[0]
        start(sum_y)
        seg0.fold_y(1, 0)
        out.pass_on(1)
        seg0.fold_y(1, 1)
        recv(sum_y)
        sums_ref[2] = sums_ref[1] + sumland_ref[1]
        start(sum_z)
        seg0.fold_z(1)
        recv(sum_z)
        sums_ref[3] = (sums_ref[2] + sumland_ref[2]) + (sumland_ref[3] + sumland_ref[4])
        start(sum_x)
        part1_ref[...] = seg1.total()
        part2_ref[...] = seg2.total()
        seg0.send_x()
        partw_ref[...] = segw.total()
        layer.finish()
        out.pass_on(0)
        recv(sum_x)
        total_ref[...] = sums_ref[3] + sumland_ref[5]
        part0_ref[...] = seg0.total()
        out.finish()
        links.sent(corew[0], core0[0])


def group_and_block(t):
    early = t < 8
    return (
        jnp.where(early, 1 - t // 4, 3 - t % 2),
        3 - jnp.where(early, t % 4, jnp.maximum(t - 8, 0) // 2),
    )


def run_fused_backward(
    tokens, gq, gw, rows, dh1, gb, gbt, q, v, kt, p, scale, o, a1t, layer, fold, work, early
):
    groups, n, _ = tokens.shape
    width = gw.shape[-1]
    heads = width // HEAD_DIM
    hidden = fold.shape[-1]
    depth = D // (Z_DEV * Y_DEV)
    step = n // 4

    def by_group(*shape):
        return pl.BlockSpec(
            (1,) + shape, lambda t: (group_and_block(t)[0],) + (0,) * len(shape)
        )

    p_spec = pl.BlockSpec(
        (1, heads, n, step),
        lambda t: (group_and_block(t)[0], 0, 0, group_and_block(t)[1]),
    )

    def early_group(*shape):
        return pl.BlockSpec(
            (1,) + shape, lambda t: (group_and_block(jnp.minimum(t, 9))[0],) + (0,) * len(shape)
        )

    copies = 2 * 12 + 4 + 2 * 15 + 2 * 11 + 6

    def landing(lanes):
        return [
            pltpu.VMEM((2, Z_DEV, depth, lanes), BF16),
            pltpu.VMEM((2, 3, depth, lanes), BF16), pltpu.VMEM((2, 2, depth, lanes), BF16),
            pltpu.VMEM((depth, lanes), BF16), pltpu.VMEM((depth, lanes), BF16),
        ]

    def working(lanes):
        block = (Z_DEV, Y_DEV, depth, lanes)
        return [pltpu.VMEM(block, BF16)] + [pltpu.VMEM((2,) + block, BF16)] * 2

    return pl.pallas_call(
        fused_backward,
        grid=(4 * groups,),
        in_specs=[
            ANY_WHOLE, by_group(D, 3 * width), early_group(D, width), VMEM_WHOLE,
            pl.BlockSpec((step, D), lambda t: (group_and_block(jnp.maximum(t, 8))[1], 0)),
            VMEM_WHOLE, ANY_WHOLE, by_group(n, width), by_group(n, width),
            by_group(width, n), p_spec, early_group(8, n), early_group(n, width),
            ANY_WHOLE, ANY_WHOLE, ANY_WHOLE, ANY_WHOLE, VMEM_WHOLE,
        ],
        out_specs=[ANY_WHOLE] * 2 + [VMEM_WHOLE] * 5,
        out_shape=[
            shaped(BF16, groups, n, D), shaped(BF16, groups, n, D),
            shaped(F32, depth, 3 * width),
            shaped(F32, depth, width), shaped(F32, depth, hidden),
            shaped(F32, depth, hidden), shaped(F32, 16, D),
        ],
        scratch_shapes=[
            pltpu.VMEM((D, n), BF16), pltpu.VMEM((D, n), BF16), pltpu.VMEM((n, D), BF16),
            pltpu.VMEM((2, Z_DEV, depth, hidden), BF16),
            pltpu.VMEM((2, Z_DEV, Y_DEV, depth, hidden), BF16),
            pltpu.VMEM((2, n, width), BF16),
            pltpu.VMEM((2, 8, n), F32), pltpu.VMEM((2, 2, n, width), F32),
            pltpu.VMEM((2, n, 3 * width), BF16), pltpu.VMEM((n, D), F32),
            pltpu.VMEM((n, D), BF16), pltpu.VMEM((n, D), BF16), pltpu.VMEM((n, D), BF16),
            pltpu.VMEM((groups, 8, width), F32),
        ]
        + landing(hidden)[:1] + landing(hidden) + landing(hidden)
        + working(width) + landing(width)
        + working(3 * width) + landing(3 * width)
        + [
            pltpu.VMEM((4, 16, D), F32), pltpu.VMEM((6, 16, D), F32),
            pltpu.SemaphoreType.DMA((copies,)), pltpu.SemaphoreType.DMA((copies,)),
            pltpu.SemaphoreType.DMA((6,)), pltpu.SemaphoreType.DMA((2, 2, 4)),
        ],
        compiler_params=pltpu.CompilerParams(
            vmem_limit_bytes=VMEM_LIMIT, collective_id=2, has_side_effects=True
        ),
        name="fused_backward",
    )(tokens, gq, gw, rows, dh1, gb, gbt, q, v, kt, p, scale, o, a1t, layer, fold, work, early)


def place_gradients(
    tie_ref, sums_ref, part0_ref, partw_ref, part1_ref, part2_ref, near_out_ref,
    near_grad_ref, far_out_ref, far_grad_ref, gains_ref, bias_ref, in_ref, out_ref, expand_ref,
    project_ref,
):
    far_out_ref[...] = near_out_ref[...]
    far_grad_ref[...] = near_grad_ref[...]
    own = gains_ref.shape[-1]
    width = partw_ref.shape[-1]

    @pl.when(pl.program_id(0) == 0)
    def _():
        first = (lax.axis_index("dp") * 4 + lax.axis_index("tensor")) * own
        feature = lax.broadcasted_iota(jnp.int32, (D, 128), 0)
        lane = lax.broadcasted_iota(jnp.int32, (D, 128), 1)
        chosen = ((feature == first + lane) & (lane < own)).astype(F32)
        sums = lax.dot_general(
            sums_ref[...], chosen, (((1,), (0,)), ((), ())),
            precision=lax.Precision.HIGHEST, preferred_element_type=F32,
        )[:, :own]
        s0, s1, s2, s3 = tie_ref[0], tie_ref[1], tie_ref[2], tie_ref[3]
        w_out = partw_ref[...].T

        def at(source, wanted, value):
            return jnp.where(source == wanted, value, jnp.zeros_like(value))

        row = lax.broadcasted_iota(jnp.int32, (NSRC, own), 0)
        for i, wanted in enumerate([s0, s0, s0, s1, s2, s3, s2, s2, s2, s2]):
            bias_ref[i] = jnp.where(row == wanted, sums[2 + i : 3 + i], 0.0)
        for s in range(NSRC):
            gains_ref[s, 0:1] = at(s, s0, sums[0:1])
            gains_ref[s, 1:2] = at(s, s2, sums[1:2])
            for j in range(3):
                in_ref[s, j] = at(s, s0, part0_ref[:, j * width : (j + 1) * width])
            out_ref[s] = at(s, s1, w_out)
            expand_ref[s] = at(s, s2, part1_ref[...])
            project_ref[s] = at(s, s3, part2_ref[...])


def run_place_gradients(tie, sums, part0, partw, part1, part2, out, grad, like):
    slots, n, _ = grad.shape
    gains, biases, w_in, w_out, w_expand, w_project = [item.shape for item in like]
    shapes = [
        gains, (biases[1], biases[0], biases[2]), w_in, w_out, w_expand,
        (w_project[0], w_project[2], w_project[1]),
    ]
    out, grad, gains, biases, w_in, w_out, w_expand, w_project = pl.pallas_call(
        place_gradients,
        grid=(slots,),
        in_specs=[SMEM_WHOLE] + [VMEM_WHOLE] * 5
        + [group(n, D), group(n, D)],
        out_specs=[group(n, D), group(n, D)] + [VMEM_WHOLE] * 6,
        out_shape=[shaped(BF16, slots, n, D)] * 2 + [shaped(F32, *item) for item in shapes],
        compiler_params=pltpu.CompilerParams(vmem_limit_bytes=VMEM_LIMIT),
        name="place_gradients",
    )(tie, sums, part0, partw, part1, part2, out, grad)
    biases = biases.transpose(1, 0, 2)
    return out, grad, gains, biases, w_in, w_out, w_expand, w_project.transpose(0, 2, 1)


def plain_step(
    tokens, lengths, tie_map, norm_gains, bias_rows, attention_in, attention_out,
    expand_weight, project_weight, cotangent,
):
    slot_rows = tokens.shape[0] // lengths.shape[0]
    me = lax.axis_index("tensor")
    in_local = lax.dynamic_index_in_dim(attention_in, tie_map[0], 0, keepdims=False)
    out_local = lax.dynamic_index_in_dim(attention_out, tie_map[1], 0, keepdims=False)
    expand_local = lax.dynamic_index_in_dim(expand_weight, tie_map[2], 0, keepdims=False)
    project_local = lax.dynamic_index_in_dim(project_weight, tie_map[3], 0, keepdims=False)
    local0 = jnp.concatenate([in_local, out_local.T[None]], 0)
    row_kinds = jnp.array([0, 0, 0, 1, 2, 3] + [2] * (FF // D), dtype=jnp.int32)
    gain_kinds = jnp.array([0, 2], dtype=jnp.int32)
    gain_pick = norm_gains[tie_map[gain_kinds], jnp.arange(2)]
    bias_pick = bias_rows[tie_map[row_kinds], jnp.arange(row_kinds.shape[0])]
    vectors = jnp.concatenate([gain_pick, bias_pick], 0)
    x = lax.dynamic_slice_in_dim(tokens, me * slot_rows, slot_rows, 0)
    cot = lax.dynamic_slice_in_dim(cotangent, me * slot_rows, slot_rows, 0)
    length = lax.dynamic_slice_in_dim(lengths, me, 1, 0)
    rows = lax.all_gather(vectors, ("dp", "tensor"), axis=1, tiled=True).astype(F32)
    rows = jnp.concatenate([rows, jnp.zeros((4, D), F32)], 0)

    def gathered(piece, axis):
        piece = lax.all_gather(piece, "dp", axis=axis, tiled=True)
        return lax.all_gather(piece, "tensor", axis=0)

    g0 = gathered(local0, 1)
    g1 = gathered(expand_local, 0)
    g2 = gathered(project_local.T, 0)
    groups, width = g0.shape[0], g0.shape[-1]
    bqv = rows[3:5].reshape(2, groups, width).transpose(1, 0, 2)
    q, v, kt, p, o, a1t, h1, a2, a2t = run_attention_forward(length, x, g0, rows, bqv)
    out, d1, d2, dh1, gb, gbt, sums = run_feed_forward(length, cot, a2, a2t, h1, g1, g2, rows)
    d0, xg, sums_in, sums_qv = run_attention_backward(
        x, g0, rows, dh1, gb, gbt, q, v, kt, p, o, a1t
    )
    layer_out = lax.all_gather(out, "tensor", axis=0, tiled=True)
    tokens_grad = lax.all_gather(xg, "tensor", axis=0, tiled=True)

    def scattered(piece, axis):
        piece = lax.psum_scatter(piece, "tensor", scatter_dimension=0)
        return lax.psum_scatter(piece, "dp", scatter_dimension=axis, tiled=True).astype(F32)

    part0 = scattered(d0, 1)
    part1 = scattered(d1, 0)
    part2 = scattered(d2, 0)
    qv = sums_qv[:, :2].transpose(1, 0, 2).reshape(2, D)
    sums = jnp.concatenate(
        [sums_in[0:1], sums[1:2], sums_in[1:2], qv, sums[5:12]], 0
    )
    sums = lax.psum_scatter(sums, ("dp", "tensor"), scatter_dimension=1, tiled=True)
    return layer_out, tokens_grad, *placed(tie_map, sums, part0, part1, part2)


def fused_step(
    tokens, lengths, tie_map, norm_gains, bias_rows, attention_in, attention_out,
    expand_weight, project_weight, cotangent,
):
    slots = lengths.shape[0]
    tokens = tokens.reshape(slots, -1, D)
    cotangent = cotangent.reshape(slots, -1, D)
    gq, gw, g1, g2, rows, q, v, kt, p, scale, o, a1t, h1, a2, a2t = run_fused_forward(
        tie_map, lengths, tokens, norm_gains, bias_rows, attention_in, attention_out,
        expand_weight, project_weight,
    )
    layer, fold, work, dh1, gb, gbt, early = run_fused_feed_forward(
        lengths, cotangent, a2, a2t, h1, g1, g2, rows
    )
    grad, out, part0, partw, part1, part2, sums = run_fused_backward(
        tokens, gq, gw, rows, dh1, gb, gbt, q, v, kt, p, scale, o, a1t, layer, fold,
        work, early,
    )
    out, grad, *placed_grads = run_place_gradients(
        tie_map, sums, part0, partw, part1, part2, out, grad,
        (norm_gains, bias_rows, attention_in, attention_out, expand_weight, project_weight),
    )
    return out.reshape(-1, D), grad.reshape(-1, D), *placed_grads


def placed(tie_map, sums, part0, part1, part2):
    source = jnp.arange(NSRC, dtype=jnp.int32)

    def place(piece, which):
        pick = (source == tie_map[which]).reshape((NSRC,) + (1,) * piece.ndim)
        return jnp.where(pick, piece[None], 0.0)

    def place_rows(piece, kinds):
        pick = source[:, None] == tie_map[jnp.array(kinds, dtype=jnp.int32)][None, :]
        return jnp.where(pick[:, :, None], piece[None], 0.0)

    return (
        place_rows(sums[:2], [0, 2]),
        place_rows(sums[2:], [0, 0, 0, 1, 2, 3] + [2] * (FF // D)),
        place(part0[:3], 0),
        place(part0[3].T, 1),
        place(part1, 2),
        place(part2.T, 3),
    )


def solution(mesh):
    fused = mesh.shape["dp"] == Z_DEV * Y_DEV and mesh.shape["tensor"] == X_DEV * C_DEV
    return jax.shard_map(
        fused_step if fused else plain_step,
        mesh=mesh,
        in_specs=(
            P("dp", None),
            P("dp"),
            P(),
            P(None, None, ("dp", "tensor")),
            P(None, None, ("dp", "tensor")),
            P(None, None, "dp", "tensor"),
            P(None, "tensor", "dp"),
            P(None, "dp", "tensor"),
            P(None, "tensor", "dp"),
            P("dp", None),
        ),
        out_specs=(
            P("dp", None),
            P("dp", None),
            P(None, None, ("dp", "tensor")),
            P(None, None, ("dp", "tensor")),
            P(None, None, "dp", "tensor"),
            P(None, "tensor", "dp"),
            P(None, "dp", "tensor"),
            P(None, "tensor", "dp"),
        ),
        check_vma=False,
    )
```

```python
import jax
import jax.numpy as jnp
from jax import lax
from jax.experimental import pallas as pl
from jax.experimental.pallas import tpu as pltpu
from jax.sharding import PartitionSpec as P

D = 768
HEAD_DIM = 64
FF = 3072
NSRC = 4
EPS = 1e-05
MASKED = -1e30
F32 = jnp.float32
BF16 = jnp.bfloat16
VMEM_LIMIT = 60 * 1024 * 1024


def dot_nn(a, b):
    return lax.dot_general(a, b, (((1,), (0,)), ((), ())), preferred_element_type=F32)


def dot_nt(a, b):
    return lax.dot_general(a, b, (((1,), (1,)), ((), ())), preferred_element_type=F32)


def norm_parts(v):
    center = jnp.mean(v, -1, keepdims=True)
    centered = v - center
    r = lax.rsqrt(jnp.mean(centered * centered, -1, keepdims=True) + EPS)
    return centered * r, r


def head_mask(shape, h):
    lane = lax.broadcasted_iota(jnp.int32, shape, 1)
    return (lane >= h * HEAD_DIM) & (lane < (h + 1) * HEAD_DIM)


def blocks(total, size):
    return [slice(i * size, (i + 1) * size) for i in range(total // size)]


def attention_forward(
    len_ref, x_ref, g_ref, rows_ref, bqv_ref,
    q_ref, v_ref, kt_ref, p_ref, o_ref, a1t_ref, h1_ref, a2_ref, a2t_ref,
    a1_ref, k_ref, vt_ref, ot_ref, attn_ref,
):
    t = pl.program_id(0)
    n = x_ref.shape[0]
    width = g_ref.shape[-1]
    heads = width // HEAD_DIM
    step = 256
    length = len_ref[0]

    @pl.when(t == 0)
    def _():
        @pl.loop(0, n // step)
        def _(b):
            rows = pl.ds(pl.multiple_of(b * step, step), step)
            xhat, _ = norm_parts(x_ref[rows, :].astype(F32))
            a1 = xhat * rows_ref[0:1, :] + rows_ref[2:3, :]
            a1_ref[rows, :] = a1.astype(BF16)
            a1t_ref[:, rows] = a1.astype(BF16).T
            attn_ref[rows, :] = x_ref[rows, :].astype(F32) + rows_ref[5:6, :]

    @pl.loop(0, n // step)
    def _(b):
        rows = pl.ds(pl.multiple_of(b * step, step), step)
        a1 = a1_ref[rows, :]
        q = (dot_nn(a1, g_ref[0, 0]) + bqv_ref[0, 0:1, :]).astype(BF16)
        q_ref[0, rows, :] = q * jnp.asarray(HEAD_DIM ** -0.5, BF16)
        k = dot_nn(a1, g_ref[0, 1]).astype(BF16)
        k_ref[rows, :] = k
        kt_ref[0, :, rows] = k.T
        v = (dot_nn(a1, g_ref[0, 2]) + bqv_ref[0, 1:2, :]).astype(BF16)
        v_ref[0, rows, :] = v
        vt_ref[:, rows] = v.T

    for h in range(heads):
        k = k_ref[...]
        k = jnp.where(head_mask(k.shape, h), k, jnp.zeros_like(k))
        for b in range(n // step):
            first, last = b * step, (b + 1) * step
            q = q_ref[0, first:last, :]
            key = lax.broadcasted_iota(jnp.int32, (last, step), 0)
            query = lax.broadcasted_iota(jnp.int32, (step, step), 1) + first
            s = dot_nt(k[:last], q)
            near = jnp.where(
                (key[first:] <= query) & (key[first:] < length), s[first:], MASKED
            )
            if b:
                far = jnp.where(key[:first] < length, s[:first], MASKED)
                top = jnp.maximum(
                    jnp.max(far, 0, keepdims=True), jnp.max(near, 0, keepdims=True)
                )
                e_far = jnp.exp(far - top)
                e_near = jnp.exp(near - top)
                total = jnp.sum(e_far, 0, keepdims=True) + jnp.sum(e_near, 0, keepdims=True)
                scale = 1.0 / total
                p_ref[0, h, :first, first:last] = (e_far * scale).astype(BF16)
            else:
                top = jnp.max(near, 0, keepdims=True)
                e_near = jnp.exp(near - top)
                scale = 1.0 / jnp.sum(e_near, 0, keepdims=True)
            p_ref[0, h, first:last, first:last] = (e_near * scale).astype(BF16)
            ot_ref[h * HEAD_DIM : (h + 1) * HEAD_DIM, first:last] = dot_nn(
                vt_ref[h * HEAD_DIM : (h + 1) * HEAD_DIM, :last],
                p_ref[0, h, :last, first:last],
            ).astype(BF16)

    @pl.loop(0, n // step)
    def _(b):
        rows = pl.ds(pl.multiple_of(b * step, step), step)
        o = ot_ref[:, rows].T
        o_ref[0, rows, :] = o
        attn_ref[rows, :] += dot_nt(o, g_ref[0, 3])

    @pl.when(t == pl.num_programs(0) - 1)
    def _():
        @pl.loop(0, n // step)
        def _(b):
            rows = pl.ds(pl.multiple_of(b * step, step), step)
            h1 = attn_ref[rows, :]
            h1_ref[rows, :] = h1
            xhat, _ = norm_parts(h1)
            a2 = (xhat * rows_ref[1:2, :] + rows_ref[6:7, :]).astype(BF16)
            a2_ref[rows, :] = a2
            a2t_ref[:, rows] = a2.T


SQRT_2_PI = 0.7978845608028654


def feed_forward_both(
    len_ref, c_ref, a2_ref, a2t_ref, h1_ref, w1_ref, w2_ref, rows_ref,
    out_ref, d1_ref, d2_ref, dh1_ref, gb_ref, gbt_ref, sums_ref,
    gf_ref, gft_ref, feed_ref, da2_ref, h_ref, df_ref,
):
    t = pl.program_id(0)
    n = c_ref.shape[0]
    step = 256
    length = len_ref[0]

    @pl.when(t == 0)
    def _():
        sums_ref[...] = jnp.zeros_like(sums_ref)

        @pl.loop(0, n // step)
        def _(b):
            rows = pl.ds(pl.multiple_of(b * step, step), step)
            place = b * step + lax.broadcasted_iota(jnp.int32, (step, 1), 0)
            live = (place < length).astype(F32)
            g = (c_ref[rows, :].astype(F32) * live).astype(BF16)
            gf_ref[rows, :] = g
            gft_ref[:, rows] = g.T
            sums_ref[7:8, :] += jnp.sum(g.astype(F32), 0, keepdims=True)

    bias = rows_ref[pl.ds(8 + t, 1), :]

    @pl.loop(0, n // step)
    def _(b):
        rows = pl.ds(pl.multiple_of(b * step, step), step)
        f = dot_nn(a2_ref[rows, :], w1_ref[0]) + bias
        dh = dot_nn(gf_ref[rows, :], w2_ref[0])
        f2 = f * f
        th = jnp.tanh(f * (SQRT_2_PI + (SQRT_2_PI * 0.044715) * f2))
        half = 0.5 + 0.5 * th
        h = (f * half).astype(BF16)
        slope = half + f * (0.5 - 0.5 * th * th) * (
            SQRT_2_PI + (3 * SQRT_2_PI * 0.044715) * f2
        )
        df = (dh * slope).astype(BF16)
        h_ref[rows, :] = h
        df_ref[rows, :] = df
        sums_ref[pl.ds(8 + t, 1), :] += jnp.sum(df.astype(F32), 0, keepdims=True)
        feed = dot_nt(h, w2_ref[0])
        da2 = dot_nt(df, w1_ref[0])

        @pl.when(t == 0)
        def _():
            feed_ref[rows, :] = feed
            da2_ref[rows, :] = da2

        @pl.when(t > 0)
        def _():
            feed_ref[rows, :] += feed
            da2_ref[rows, :] += da2

    @pl.loop(0, D // step)
    def _(b):
        rows = pl.ds(pl.multiple_of(b * step, step), step)
        d1_ref[0, rows, :] = dot_nn(a2t_ref[rows, :], df_ref[...]).astype(BF16)
        d2_ref[0, rows, :] = dot_nn(gft_ref[rows, :], h_ref[...]).astype(BF16)

    @pl.when(t == pl.num_programs(0) - 1)
    def _():
        @pl.loop(0, n // step)
        def _(b):
            rows = pl.ds(pl.multiple_of(b * step, step), step)
            place = b * step + lax.broadcasted_iota(jnp.int32, (step, 1), 0)
            live = (place < length).astype(F32)
            h1 = h1_ref[rows, :]
            out_ref[rows, :] = (live * (h1 + (feed_ref[rows, :] + rows_ref[7:8, :]))).astype(BF16)
            xhat, r = norm_parts(h1)
            da2 = da2_ref[rows, :]
            sums_ref[1:2, :] += jnp.sum(da2 * xhat, 0, keepdims=True)
            sums_ref[6:7, :] += jnp.sum(da2, 0, keepdims=True)
            dg = da2 * rows_ref[1:2, :]
            dv = r * (
                dg
                - jnp.mean(dg, -1, keepdims=True)
                - xhat * jnp.mean(dg * xhat, -1, keepdims=True)
            )
            dh1 = live * c_ref[rows, :].astype(F32) + dv
            dh1_ref[rows, :] = dh1
            gb = dh1.astype(BF16)
            gb_ref[rows, :] = gb
            gbt_ref[:, rows] = gb.T
            sums_ref[5:6, :] += jnp.sum(gb.astype(F32), 0, keepdims=True)


def attention_backward(
    x_ref, g_ref, rows_ref, dh1_ref, gb_ref, gbt_ref, q_ref, v_ref, kt_ref, p_ref,
    o_ref, a1t_ref,
    d0_ref, xg_ref, sums_ref, bqv_ref,
    do_ref, delta_ref, dqt_ref, dq_ref, dk_ref, dv_ref, da1_ref,
):
    t = pl.program_id(0)
    n = x_ref.shape[0]
    width = g_ref.shape[-1]
    heads = width // HEAD_DIM
    step = 256
    pick = (
        lax.broadcasted_iota(jnp.int32, (16, width), 1) // HEAD_DIM
        == lax.broadcasted_iota(jnp.int32, (16, width), 0)
    ).astype(BF16)

    @pl.loop(0, n // step)
    def _(b):
        rows = pl.ds(pl.multiple_of(b * step, step), step)
        do = dot_nn(gb_ref[rows, :], g_ref[0, 3]).astype(BF16)
        do_ref[rows, :] = do
        prod = do.astype(F32) * o_ref[0, rows, :].astype(F32)
        high = prod.astype(BF16)
        low = (prod - high.astype(F32)).astype(BF16)
        delta_ref[:, rows] = dot_nt(pick, high) + dot_nt(pick, low)

    dqt_ref[...] = jnp.zeros_like(dqt_ref)
    for b in range(n // step):
        first, last = b * step, (b + 1) * step
        do = do_ref[first:, :]
        q = q_ref[0, first:, :]
        v = v_ref[0, first:last, :]
        dk, dv = None, None
        for h in range(heads):
            mine = head_mask((1, width), h)
            zero = jnp.zeros((), BF16)
            p = p_ref[0, h, first:last, first:]
            dp = dot_nt(jnp.where(mine, v, zero), do)
            ds = (p.astype(F32) * (dp - delta_ref[h : h + 1, first:])).astype(BF16)
            part = dot_nn(p, jnp.where(mine, do, zero))
            dv = part if dv is None else dv + part
            part = dot_nn(ds, jnp.where(mine, q, zero))
            dk = part if dk is None else dk + part
            head = slice(h * HEAD_DIM, (h + 1) * HEAD_DIM)
            dqt_ref[head, first:] += dot_nn(kt_ref[0, head, first:last], ds)
        dk_ref[first:last, :] = dk.astype(BF16)
        dv_ref[first:last, :] = dv.astype(BF16)

    @pl.when(t == 0)
    def _():
        da1_ref[...] = jnp.zeros_like(da1_ref)

    bqv_ref[...] = jnp.zeros_like(bqv_ref)

    @pl.loop(0, n // step)
    def _(b):
        rows = pl.ds(pl.multiple_of(b * step, step), step)
        dq = (dqt_ref[:, rows] * HEAD_DIM ** -0.5).astype(BF16).T
        dk = dk_ref[rows, :]
        dv = dv_ref[rows, :]
        dq_ref[rows, :] = dq
        bqv_ref[0, 0:1, :] += jnp.sum(dq.astype(F32), 0, keepdims=True)
        bqv_ref[0, 1:2, :] += jnp.sum(dv.astype(F32), 0, keepdims=True)
        da1_ref[rows, :] += (
            dot_nt(dq, g_ref[0, 0]) + dot_nt(dk, g_ref[0, 1]) + dot_nt(dv, g_ref[0, 2])
        )

    @pl.loop(0, D // step)
    def _(b):
        rows = pl.ds(pl.multiple_of(b * step, step), step)
        a1t = a1t_ref[rows, :]
        d0_ref[0, 0, rows, :] = dot_nn(a1t, dq_ref[...]).astype(BF16)
        d0_ref[0, 1, rows, :] = dot_nn(a1t, dk_ref[...]).astype(BF16)
        d0_ref[0, 2, rows, :] = dot_nn(a1t, dv_ref[...]).astype(BF16)
        d0_ref[0, 3, rows, :] = dot_nn(gbt_ref[rows, :], o_ref[0]).astype(BF16)

    @pl.when(t == pl.num_programs(0) - 1)
    def _():
        sums_ref[...] = jnp.zeros_like(sums_ref)

        @pl.loop(0, n // step)
        def _(b):
            rows = pl.ds(pl.multiple_of(b * step, step), step)
            xhat, r = norm_parts(x_ref[rows, :].astype(F32))
            da1 = da1_ref[rows, :]
            sums_ref[0:1, :] += jnp.sum(da1 * xhat, 0, keepdims=True)
            sums_ref[1:2, :] += jnp.sum(da1, 0, keepdims=True)
            dg = da1 * rows_ref[0:1, :]
            dv = r * (
                dg
                - jnp.mean(dg, -1, keepdims=True)
                - xhat * jnp.mean(dg * xhat, -1, keepdims=True)
            )
            xg_ref[rows, :] = (dh1_ref[rows, :] + dv).astype(BF16)


def whole(*shape):
    return pl.BlockSpec(shape, lambda t: (0,) * len(shape))


def group(*shape):
    return pl.BlockSpec((1,) + shape, lambda t: (t,) + (0,) * len(shape))


def shaped(dtype, *shape):
    return jax.ShapeDtypeStruct(shape, dtype)


SMEM_WHOLE = pl.BlockSpec(memory_space=pltpu.SMEM)


def run_attention_forward(length, x, g0, rows, bqv):
    n = x.shape[0]
    groups, _, _, width = g0.shape
    heads = width // HEAD_DIM
    return pl.pallas_call(
        attention_forward,
        grid=(groups,),
        in_specs=[SMEM_WHOLE, whole(n, D), group(4, D, width), whole(16, D), group(2, width)],
        out_specs=[
            group(n, width), group(n, width), group(width, n), group(heads, n, n),
            group(n, width), whole(D, n), whole(n, D), whole(n, D), whole(D, n),
        ],
        out_shape=[
            shaped(BF16, groups, n, width), shaped(BF16, groups, n, width),
            shaped(BF16, groups, width, n), shaped(BF16, groups, heads, n, n),
            shaped(BF16, groups, n, width), shaped(BF16, D, n), shaped(F32, n, D),
            shaped(BF16, n, D), shaped(BF16, D, n),
        ],
        scratch_shapes=[
            pltpu.VMEM((n, D), BF16), pltpu.VMEM((n, width), BF16),
            pltpu.VMEM((width, n), BF16), pltpu.VMEM((width, n), BF16),
            pltpu.VMEM((n, D), F32),
        ],
        compiler_params=pltpu.CompilerParams(vmem_limit_bytes=VMEM_LIMIT),
        name="attention_forward",
    )(length, x, g0, rows, bqv)


def run_feed_forward(length, cot, a2, a2t, h1, g1, g2, rows):
    n = cot.shape[0]
    groups, _, width = g1.shape
    return pl.pallas_call(
        feed_forward_both,
        grid=(groups,),
        in_specs=[
            SMEM_WHOLE, whole(n, D), whole(n, D), whole(D, n), whole(n, D),
            group(D, width), group(D, width), whole(16, D),
        ],
        out_specs=[
            whole(n, D), group(D, width), group(D, width), whole(n, D), whole(n, D),
            whole(D, n), whole(16, D),
        ],
        out_shape=[
            shaped(BF16, n, D), shaped(BF16, groups, D, width), shaped(BF16, groups, D, width),
            shaped(F32, n, D), shaped(BF16, n, D), shaped(BF16, D, n), shaped(F32, 16, D),
        ],
        scratch_shapes=[
            pltpu.VMEM((n, D), BF16), pltpu.VMEM((D, n), BF16), pltpu.VMEM((n, D), F32),
            pltpu.VMEM((n, D), F32), pltpu.VMEM((n, width), BF16), pltpu.VMEM((n, width), BF16),
        ],
        compiler_params=pltpu.CompilerParams(vmem_limit_bytes=VMEM_LIMIT),
        name="feed_forward_both",
    )(length, cot, a2, a2t, h1, g1, g2, rows)


def run_attention_backward(x, g0, rows, dh1, gb, gbt, q, v, kt, p, o, a1t):
    n = x.shape[0]
    groups, _, _, width = g0.shape
    heads = width // HEAD_DIM
    return pl.pallas_call(
        attention_backward,
        grid=(groups,),
        in_specs=[
            whole(n, D), group(4, D, width), whole(16, D), whole(n, D), whole(n, D),
            whole(D, n), group(n, width), group(n, width), group(width, n),
            group(heads, n, n), group(n, width), whole(D, n),
        ],
        out_specs=[group(4, D, width), whole(n, D), whole(8, D), group(8, width)],
        out_shape=[
            shaped(BF16, groups, 4, D, width), shaped(BF16, n, D), shaped(F32, 8, D),
            shaped(F32, groups, 8, width),
        ],
        scratch_shapes=[
            pltpu.VMEM((n, width), BF16), pltpu.VMEM((16, n), F32), pltpu.VMEM((width, n), F32),
            pltpu.VMEM((n, width), BF16), pltpu.VMEM((n, width), BF16),
            pltpu.VMEM((n, width), BF16), pltpu.VMEM((n, D), F32),
        ],
        compiler_params=pltpu.CompilerParams(vmem_limit_bytes=VMEM_LIMIT),
        name="attention_backward",
    )(x, g0, rows, dh1, gb, gbt, q, v, kt, p, o, a1t)


Z_DEV, Y_DEV, X_DEV, C_DEV = 4, 2, 2, 2


class Place:
    def __init__(self):
        dp, self.t = lax.axis_index("dp"), lax.axis_index("tensor")
        self.dp = dp
        self.z, self.y = dp // 2, dp % 2
        self.x, self.c = self.t // 2, self.t % 2
        self.other_y = 1 - self.y
        self.zs = [
            self.z,
            self.z + 1 - 2 * (self.z % 2),
            self.z + 2 - 4 * (self.z // 2),
            3 - self.z,
        ]
        self.ts = [
            self.t,
            self.t + 1 - 2 * (self.t % 2),
            self.t + 2 - 4 * (self.t // 2),
            3 - self.t,
        ]
        self.to_z = [dict(dp=z * 2 + self.y) for z in self.zs]
        self.to_y = dict(dp=self.z * 2 + self.other_y)
        self.to_x = dict(tensor=self.ts[2])
        self.same_t = self.to_z[1:] + [dict(dp=z * 2 + self.other_y) for z in self.zs]
        self.same_dp = [dict(tensor=t) for t in self.ts[1:]]
        self.to_core = dict(tensor=self.ts[1])

    def group(self, k):
        return lax.select(
            k == 0, self.ts[0],
            lax.select(k == 1, self.ts[1], lax.select(k == 2, self.ts[2], self.ts[3])),
        )

    def greet(self, others=None):
        barrier = pltpu.get_barrier_semaphore()
        others = others or self.to_z[1:] + [self.to_y, self.to_x, self.to_core]
        for device in others:
            pl.semaphore_signal(
                barrier, inc=1, device_id=device, device_id_type=pl.DeviceIdType.MESH
            )
        pl.semaphore_wait(barrier, len(others))


class Links:
    def __init__(self, send_sem, recv_sem):
        self.send_sem, self.recv_sem = send_sem, recv_sem
        self.copies = []

    def add(self, device, src, dst):
        number = len(self.copies)
        copy = pltpu.make_async_remote_copy(
            src_ref=src,
            dst_ref=dst,
            send_sem=self.send_sem.at[number],
            recv_sem=self.recv_sem.at[number],
            device_id=device,
            device_id_type=pl.DeviceIdType.MESH,
        )
        self.copies.append(copy)
        return copy

    def sent(self, *apart):
        for copy in self.copies:
            if all(copy is not other for other in apart):
                copy.wait_send()


def flat(copies):
    for item in copies:
        if isinstance(item, list):
            yield from flat(item)
        else:
            yield item


def start(*copies):
    for copy in flat(copies):
        copy.start()


def recv(*copies):
    for copy in flat(copies):
        copy.wait_recv()


class Gather:
    def __init__(self, links, place, own, full, order, single=True, last=True):
        every = slice(None)
        y, other = place.y, place.other_y

        def same(device, k, yy, to):
            return links.add(device, full(k, every, yy), full(to, every, yy))

        def along_z(k, yy, block):
            here, passed = full(k, place.z, yy), full(k, place.zs[2], yy)
            return [
                links.add(place.to_z[1], block, here),
                links.add(place.to_z[2], block, here),
                links.add(place.to_z[1], passed, passed),
            ]

        self.z = along_z(0, y, own)
        if order == X_Z_Y:
            self.first = [links.add(place.to_x, own, full(2, place.z, y))]
            self.far = along_z(2, y, full(2, place.z, y))
            blocks = [(0, y), (2, y), (0, other), (2, other)]
        else:
            blocks = [(0, y), (0, other), (2, y), (2, other)]
        if order == Y_Z_X:
            self.first = [links.add(place.to_y, own, full(0, place.z, y))]
            self.far = along_z(0, other, full(0, place.z, other))
        if order == Z_Y_X and single:
            self.first = [same(place.to_y, 0, y, 0)]
        if order == Z_Y_X and not single:
            self.first = [links.add(place.to_y, own, full(0, place.z, y))]
            for k in range(1, 4):
                block = full(0, place.zs[k], y)
                self.first.append(links.add(place.to_y, block, block))
        self.second = [
            same(place.to_y, k, yy, k) if order == X_Z_Y else same(place.to_x, k, yy, 2)
            for k, yy in blocks[: 2 if last else 1]
        ]
        if not last:
            blocks = [block for block in blocks if block[0] == 0]
        self.core = [same(place.to_core, k, yy, k + 1) for k, yy in blocks]


Z_Y_X, Y_Z_X, X_Z_Y = range(3)


def fused_forward(
    tie_ref, len_ref, tokens_ref, gains_ref, bias_ref, in_ref, out_ref, expand_ref,
    project_ref,
    gq_ref, gw_ref, flat1_ref, flat2_ref, rows_ref,
    q_ref, v_ref, kt_ref, p_ref, scale_ref, o_ref, a1t_out, h1_out, a2_out, a2t_out,
    own0_ref, ownw_ref, own1_ref, own2_ref, square_ref, vec_ref,
    all0_ref, allw_ref, w1_ref, w2_ref, vecs_ref, bqv_ref, x_ref, a1_ref, k_ref, qa_ref, vt_ref, ot_ref, a1t_ref, h1_ref, a2_ref, a2t_ref,
    send_sem, recv_sem, local_sem, flush_sem, row_sem,
):
    t = pl.program_id(0)
    n, _ = x_ref.shape
    width = allw_ref.shape[-1]
    heads = width // HEAD_DIM
    step = 256
    place = Place()
    length = len_ref[place.t]
    links = Links(send_sem, recv_sem)
    z, y, x, c = place.z, place.y, place.x, place.c
    mine_there = vecs_ref.at[z, y, x, c]
    column = vecs_ref.at[:, :, x, c]
    vec_one = [links.add(device, vec_ref, mine_there) for device in place.same_t]
    vec_two = [links.add(device, column, column) for device in place.same_dp]
    seg0 = Gather(
        links, place, own0_ref, lambda k, z, y: all0_ref.at[k, z, y], Z_Y_X, single=False
    )
    segw = Gather(links, place, ownw_ref, lambda k, z, y: allw_ref.at[k, z, y], Z_Y_X)
    seg1 = Gather(
        links, place, own1_ref, lambda k, z, y: w1_ref.at[k, z, y], Y_Z_X, last=False
    )
    seg2 = Gather(
        links, place, own2_ref, lambda k, z, y: w2_ref.at[k, z, y], X_Z_Y, last=False
    )
    flush = [
        [
            pltpu.make_async_copy(ref.at[k], flat.at[k], flush_sem.at[i, k])
            for k in range(3)
        ]
        for i, (ref, flat) in enumerate([(w1_ref, flat1_ref), (w2_ref, flat2_ref)])
    ]
    put_a1t = pltpu.make_async_copy(a1t_ref, a1t_out, local_sem.at[0])
    put_a2t = pltpu.make_async_copy(a2t_ref, a2t_out, local_sem.at[1])
    puts = []
    for i in range(n // step):
        rows = pl.ds(i * step, step)
        puts.append([
            pltpu.make_async_copy(h1_ref.at[rows], h1_out.at[rows], row_sem.at[0, i]),
            pltpu.make_async_copy(a2_ref.at[rows], a2_out.at[rows], row_sem.at[1, i]),
        ])
    fetch = pltpu.make_async_copy(tokens_ref.at[place.t], x_ref, local_sem.at[2])

    def relay_z(copies):
        recv(copies[1])
        start(copies[2])

    def pass_own(seg):
        recv(seg.z[0], seg.z[2])
        if seg is segw:
            start(seg.first)
        start(seg.second[0], seg.core[0])

    def pass_second(seg):
        recv(seg.second)
        if seg is seg2:
            start(seg.core[1])

    def pass_first(seg):
        recv(seg.first)
        if seg is segw:
            start(seg.second[1], seg.core[1])
        else:
            start(seg.far[1], seg.far[0])

    def pass_far(seg):
        recv(seg.far[0], seg.far[2])
        start(seg.core[1:] if seg is seg1 else [])

    def pass_core(seg, i):
        recv(seg.second[i])
        start(seg.core[2 + i])

    plan = [
        (0, 0, lambda: (pass_own(segw), pass_first(seg1), relay_z(seg2.z), pass_first(seg2))),
        (0, 3, lambda: (pass_first(segw), relay_z(seg1.z), pass_core(seg0, 0))),
        (1, 0, lambda: recv(seg0.core[:2])),
        (1, 1, lambda: relay_z(seg1.far)),
        (1, 3, lambda: pass_core(seg0, 1)),
        (1, 4, lambda: (recv(segw.core[:2]), pass_core(segw, 0), pass_own(seg2))),
        (2, 1, lambda: relay_z(seg2.far)),
        (2, 2, lambda: pass_core(segw, 1)),
        (2, 3, lambda: pass_own(seg1)),
        (3, 0, lambda: (recv(seg0.core[2:]), pass_far(seg1), flush[0][0].start())),
        (3, 2, lambda: (pass_second(seg2), flush[1][0].start())),
        (3, 3, lambda: (pass_far(seg2), flush[1][2].start())),
        (3, 4, lambda: recv(segw.core[2:])),
    ]

    def serve(point):
        for step, where, act in plan:
            if where == point:
                pl.when(t == step)(lambda act=act: (act(), None)[1])

    @pl.when(t == 0)
    def _():
        s0, s1, s2, s3 = tie_ref[0], tie_ref[1], tie_ref[2], tie_ref[3]
        fetch.start()
        square_ref[...] = jnp.zeros_like(square_ref)
        gain = gains_ref.shape[-1]
        square_ref[0:1, :gain] = gains_ref[s0].astype(F32)[0:1]
        square_ref[1:2, :gain] = gains_ref[s2].astype(F32)[1:2]
        kinds = [s0, s0, s0, s1, s2, s3, s2, s2, s2, s2]
        for i, source in enumerate(kinds):
            wide = bias_ref[i].astype(F32)
            here = lax.broadcasted_iota(jnp.int32, wide.shape, 0) == source
            square_ref[2 + i : 3 + i, :gain] = jnp.sum(
                jnp.where(here, wide, 0.0), 0, keepdims=True
            )
        vec_ref[...] = square_ref[...].T[:gain]
        for j in range(3):
            own0_ref[:, j * width : (j + 1) * width] = in_ref[s0, j]
        place.greet(place.same_t + place.same_dp)
        start(vec_one, seg0.z[1], seg0.z[0], seg0.first[0])
        vecs_ref[z, y, x, c] = vec_ref[...]
        ones = lax.broadcasted_iota(jnp.int32, (vt_ref.shape[1] - HEAD_DIM, n), 0) == 0
        for h in range(heads):
            vt_ref[h, HEAD_DIM:, :] = ones.astype(BF16)
        all0_ref[0, z, y] = own0_ref[...]
        ownw_ref[...] = out_ref[s1].T
        allw_ref[0, z, y] = ownw_ref[...]
        own1_ref[...] = expand_ref[s2]
        own2_ref[...] = project_ref[s3]
        w1_ref[0, z, y] = own1_ref[...]
        w2_ref[0, z, y] = own2_ref[...]
        recv(vec_one)
        start(vec_two)
        relay_z(seg0.z)
        start(seg0.first[2])
        recv(seg0.z[0])
        start(seg0.first[1], segw.z[1], segw.z[0], seg2.z[1])
        recv(vec_two)
        start(seg2.first)
        vecs = vecs_ref[...].reshape(D, vecs_ref.shape[-1]).T[:16]
        rows_ref[...] = vecs
        recv(seg0.z[2])
        start(seg0.first[3], seg1.first, seg0.second[0], seg0.core[0])
        for k in range(4):
            part = slice(k * width, (k + 1) * width)
            bqv_ref[k, 0:1, :width] = vecs[3:4, part]
            bqv_ref[k, 0:1, width : 2 * width] = jnp.zeros((1, width), F32)
            bqv_ref[k, 0:1, 2 * width :] = vecs[4:5, part]
        fetch.wait()

        @pl.loop(0, n // step)
        def _(b):
            rows = pl.ds(pl.multiple_of(b * step, step), step)
            wide = x_ref[rows, :].astype(F32)
            xhat, _ = norm_parts(wide)
            a1 = (xhat * rows_ref[0:1, :] + rows_ref[2:3, :]).astype(BF16)
            a1_ref[rows, :] = a1
            a1t_ref[:, rows] = a1.T
            h1_ref[rows, :] = wide + rows_ref[5:6, :]

        put_a1t.start()
        relay_z(segw.z)
        start(seg2.z[0], seg1.z[1], seg1.z[0])
        recv(seg0.first)
        start(seg0.second[1], seg0.core[1])

    serve(0)
    gq = all0_ref[t].reshape(D, 3 * width)
    gq_ref[0] = gq
    mine = place.group(t)
    qkv = dot_nn(a1_ref[...], gq) + bqv_ref[mine, 0:1, :]
    q = qkv[:, :width].astype(BF16) * jnp.asarray(HEAD_DIM ** -0.5, BF16)
    k = qkv[:, width : 2 * width].astype(BF16)
    v = qkv[:, 2 * width :].astype(BF16)
    q_ref[0] = q
    kt_ref[0] = k.T
    v_ref[0] = v
    vt = v.T
    for h in range(heads):
        vt_ref[h, :HEAD_DIM, :] = vt[h * HEAD_DIM : (h + 1) * HEAD_DIM]
    spare = k_ref.shape[1] - width
    dead = lax.broadcasted_iota(jnp.int32, (n, spare), 0) >= length
    first_column = lax.broadcasted_iota(jnp.int32, (n, spare), 1) == 0
    k_ref[:, :width] = k
    k_ref[:, width:] = jnp.where(first_column & dead, MASKED, 0.0).astype(BF16)
    qa_ref[:, :width] = q
    qa_ref[:, width:] = jnp.where(first_column, 1.0, 0.0).astype(BF16)

    serve(1)
    def scores(h, b):
        first, last = b * step, (b + 1) * step
        q = qa_ref[first:last, :]
        lane = lax.broadcasted_iota(jnp.int32, (1, q.shape[1]), 1)
        keep = head_mask((1, q.shape[1]), h) | (lane >= width)
        return dot_nt(k_ref[:last, :], jnp.where(keep, q, jnp.zeros((), BF16)))

    def attend(h, b, s):
        first, last = b * step, (b + 1) * step
        key = lax.broadcasted_iota(jnp.int32, (step, step), 0)
        query = lax.broadcasted_iota(jnp.int32, (step, step), 1)
        near = jnp.where(key <= query, s[first:], MASKED)
        top = jnp.max(near, 0, keepdims=True)
        if b:
            far = s[:first]
            top = jnp.maximum(top, jnp.max(far, 0, keepdims=True))
        e_near = jnp.exp((near - top).astype(BF16))
        p_ref[0, h, first:last, first:last] = e_near
        o = dot_nn(vt_ref[h, :, first:last], e_near)
        if b:
            e_far = jnp.exp((far - top).astype(BF16))
            p_ref[0, h, :first, first:last] = e_far
            o += dot_nn(vt_ref[h, :, :first], e_far)
        scale = 1.0 / o[HEAD_DIM : HEAD_DIM + 1]
        scale_ref[0, h : h + 1, first:last] = scale
        ot_ref[h * HEAD_DIM : (h + 1) * HEAD_DIM, first:last] = (
            o[:HEAD_DIM] * scale
        ).astype(BF16)

    scale_ref[0, heads:, :] = jnp.zeros((scale_ref.shape[1] - heads, n), F32)
    for h in range(heads):
        s = scores(h, 0)
        for b in range(n // step):
            ahead = scores(h, b + 1) if b + 1 < n // step else None
            attend(h, b, s)
            s = ahead
        serve(2 + h)

    gw_ref[0] = allw_ref[t].reshape(gw_ref.shape[1:])
    o = ot_ref[...].T
    o_ref[0] = o
    h1_ref[...] += dot_nt(o, gw_ref[0])

    @pl.when(t == 3)
    def _():
        for i, rows in enumerate(blocks(n, step)):
            xhat, _ = norm_parts(h1_ref[rows, :])
            a2 = (xhat * rows_ref[1:2, :] + rows_ref[6:7, :]).astype(BF16)
            a2_ref[rows, :] = a2
            a2t_ref[:, rows] = a2.T
            for put in puts[i]:
                put.start()
        put_a2t.start()
        recv(seg2.core)
        flush[1][1].start()
        recv(seg1.core)
        flush[0][1].start()
        pass_second(seg1)
        flush[0][2].start()
        links.sent()
        for copies in flush + puts + [[put_a1t, put_a2t]]:
            for copy in copies:
                copy.wait()


N_GATHER = 10 + 13 + 10 + 10 + 10
VMEM_WHOLE = pl.BlockSpec(memory_space=pltpu.VMEM)
ANY_WHOLE = pl.BlockSpec(memory_space=pl.ANY)


def run_fused_forward(tie, lengths, tokens, gains, biases, w_in, w_out, w_expand, w_project):
    groups, n, _ = tokens.shape
    depth, width = w_in.shape[-2:]
    heads = width // HEAD_DIM
    hidden = w_expand.shape[-1]
    w_project = w_project.transpose(0, 2, 1)
    biases = biases.transpose(1, 0, 2)
    own = gains.shape[-1]
    return pl.pallas_call(
        fused_forward,
        grid=(groups,),
        in_specs=[SMEM_WHOLE, SMEM_WHOLE, ANY_WHOLE] + [VMEM_WHOLE] * 6,
        out_specs=[
            group(D, 3 * width), group(D, width), ANY_WHOLE, ANY_WHOLE, VMEM_WHOLE,
            group(n, width), group(n, width), group(width, n), group(heads, n, n),
            group(8, n), group(n, width), ANY_WHOLE, ANY_WHOLE, ANY_WHOLE, ANY_WHOLE,
        ],
        out_shape=[
            shaped(BF16, groups, D, 3 * width), shaped(BF16, groups, D, width),
            shaped(BF16, groups, Z_DEV, Y_DEV, depth, hidden),
            shaped(BF16, groups, Z_DEV, Y_DEV, depth, hidden),
            shaped(F32, 16, D),
            shaped(BF16, groups, n, width), shaped(BF16, groups, n, width),
            shaped(BF16, groups, width, n), shaped(BF16, groups, heads, n, n),
            shaped(F32, groups, 8, n), shaped(BF16, groups, n, width), shaped(BF16, D, n), shaped(F32, n, D),
            shaped(BF16, n, D), shaped(BF16, D, n),
        ],
        scratch_shapes=[
            pltpu.VMEM((depth, 3 * width), BF16), pltpu.VMEM((depth, width), BF16),
            pltpu.VMEM((depth, hidden), BF16), pltpu.VMEM((depth, hidden), BF16),
            pltpu.VMEM((128, 128), F32), pltpu.VMEM((own, 128), F32),
            pltpu.VMEM((groups, Z_DEV, Y_DEV, depth, 3 * width), BF16),
            pltpu.VMEM((groups, Z_DEV, Y_DEV, depth, width), BF16),
            pltpu.VMEM((groups, Z_DEV, Y_DEV, depth, hidden), BF16),
            pltpu.VMEM((groups, Z_DEV, Y_DEV, depth, hidden), BF16),
            pltpu.VMEM((Z_DEV, Y_DEV, X_DEV, C_DEV, own, 128), F32),
            pltpu.VMEM((groups, 8, 3 * width), F32),
            pltpu.VMEM((n, D), BF16), pltpu.VMEM((n, D), BF16), pltpu.VMEM((n, 256), BF16),
            pltpu.VMEM((n, 256), BF16), pltpu.VMEM((heads, HEAD_DIM + 16, n), BF16),
            pltpu.VMEM((width, n), BF16),
            pltpu.VMEM((D, n), BF16), pltpu.VMEM((n, D), F32), pltpu.VMEM((n, D), BF16),
            pltpu.VMEM((D, n), BF16),
            pltpu.SemaphoreType.DMA((N_GATHER,)), pltpu.SemaphoreType.DMA((N_GATHER,)),
            pltpu.SemaphoreType.DMA((3,)), pltpu.SemaphoreType.DMA((2, 4)),
            pltpu.SemaphoreType.DMA((2, n // 256)),
        ],
        compiler_params=pltpu.CompilerParams(
            vmem_limit_bytes=VMEM_LIMIT, collective_id=0, has_side_effects=True
        ),
        name="fused_forward",
    )(tie, lengths, tokens, gains, biases, w_in, w_out, w_expand, w_project)


class Result:
    def __init__(self, links, place, own_ref, passing_ref, out_ref, step, sem):
        count = own_ref.shape[0] // step
        self.x, self.core, self.far, self.keep, self.keep_far = [], [], [], [], []
        for i in range(count):
            rows = pl.ds(i * step, step)
            mine, theirs = out_ref.at[place.t, rows], out_ref.at[place.ts[2], rows]
            own, passing = own_ref.at[rows], passing_ref.at[rows]
            self.x.append(links.add(place.to_x, own, passing))
            self.core.append(links.add(place.to_core, own, mine))
            self.far.append(links.add(place.to_core, passing, theirs))
            self.keep.append(pltpu.make_async_copy(own, mine, sem.at[0, i]))
            self.keep_far.append(pltpu.make_async_copy(passing, theirs, sem.at[1, i]))

    def send(self, i):
        start(self.x[i], self.core[i], self.keep[i])

    def pass_on(self, i):
        recv(self.x[i])
        start(self.far[i], self.keep_far[i])

    def finish(self):
        recv(self.core, self.far)
        for copy in self.keep + self.keep_far:
            copy.wait()


def low(value):
    return jnp.asarray(value, BF16)


def pair_order(i):
    return i + 1 - 2 * (i % 2)


def fused_feed_forward(
    len_ref, cot_ref, a2_ref, a2t_in, h1_in, far1_ref, far2_ref, rows_ref,
    out_out, fold_ref, work_out, dh1_out, gb_out, gbt_out, sums_ref,
    gf_ref, gft_ref, feed_ref, da2_ref, h_ref, df_ref, weights_ref, missing_ref, third_ref,
    stage_ref, land_ref, near_ref, cross_ref, a2t_ref, h1_ref, out_ref, work_ref,
    send_sem, recv_sem, local_sem, row_sem,
):
    t = pl.program_id(0)
    n = gf_ref.shape[0]
    step = 256
    depth = stage_ref.shape[-2]
    place = Place()
    length = len_ref[place.t]
    links = Links(send_sem, recv_sem)
    y, other = place.y, place.other_y
    last = [
        links.add(place.to_x, far1_ref.at[0, :, other], missing_ref.at[0, 0]),
        links.add(place.to_y, far2_ref.at[2, :, y], missing_ref.at[1, 0]),
    ]
    last_core = [
        links.add(place.to_core, missing_ref.at[i, 0], missing_ref.at[i, 1]) for i in range(2)
    ]
    third = [
        links.add(place.to_core, far_ref.at[2, :, y], third_ref.at[i])
        for i, far_ref in enumerate([far1_ref, far2_ref])
    ]
    core = [
        [links.add(place.to_core, stage_ref.at[i], land_ref.at[s, i]) for i in range(2)]
        for s in range(2)
    ]
    cross = [
        links.add(place.to_y, near_ref.at[i, :, other], cross_ref.at[i]) for i in range(2)
    ]
    fetch = pltpu.make_async_copy(cot_ref.at[place.t], gf_ref, local_sem.at[0])
    gb_ref, gbt_ref, dh1_ref = gf_ref, gft_ref, da2_ref
    late = [
        pltpu.make_async_copy(a2t_in, a2t_ref, local_sem.at[5]),
        pltpu.make_async_copy(h1_in, h1_ref, local_sem.at[6]),
    ]
    puts = []
    for i in range(n // step):
        rows = pl.ds(i * step, step)
        puts.append([
            pltpu.make_async_copy(ref.at[rows], out.at[rows], row_sem.at[j, i])
            for j, (ref, out) in enumerate(
                [(out_ref, out_out), (dh1_ref, dh1_out), (gb_ref, gb_out)]
            )
        ])
    put_gbt = pltpu.make_async_copy(gbt_ref, gbt_out, local_sem.at[7])
    put_work = pltpu.make_async_copy(work_ref, work_out, local_sem.at[8])
    k = pair_order(t)
    mine = place.group(k)

    def load(step, whole, slot):
        for i, far_ref in enumerate([far1_ref, far2_ref]):
            group = far_ref.at[pair_order(step)]
            to = weights_ref.at[slot, i]
            if not whole:
                group, to = group.at[:, y], to.at[:, y]
            yield pltpu.make_async_copy(group, to, local_sem.at[1 + 2 * slot + i])

    def live_rows(b):
        at = b * step + lax.broadcasted_iota(jnp.int32, (step, 1), 0)
        return (at < length).astype(F32)

    @pl.when(t == 0)
    def _():
        fetch.start()
        for copy in load(0, True, 0):
            copy.start()
        for copy in late:
            copy.start()
        place.greet()
        start(last, third)
        sums_ref[...] = jnp.zeros_like(sums_ref)
        feed_ref[...] = jnp.zeros_like(feed_ref)
        da2_ref[...] = jnp.zeros_like(da2_ref)
        fetch.wait()

        @pl.loop(0, n // step)
        def _(b):
            rows = pl.ds(pl.multiple_of(b * step, step), step)
            g = (gf_ref[rows, :].astype(F32) * live_rows(b)).astype(BF16)
            gf_ref[rows, :] = g
            gft_ref[:, rows] = g.T
            sums_ref[7:8, :] += jnp.sum(g.astype(F32), 0, keepdims=True)

    for i in range(4):
        @pl.when(t == i)
        def _():
            if i == 2:
                recv(last_core, third)
            else:
                for copy in load(i, i < 2, i % 2):
                    copy.wait()
            if i in (0, 2):
                for copy in load(i + 1, i + 1 < 2, (i + 1) % 2):
                    copy.start()
            for j in range(2):
                if i == 2:
                    weights_ref[0, j, :, y] = third_ref[j]
                if i >= 2:
                    weights_ref[i % 2, j, :, other] = missing_ref[j, 3 - i]

    bias = rows_ref[pl.ds(8 + mine, 1), :]
    w1 = weights_ref[t % 2, 0].reshape(D, -1)
    w2 = weights_ref[t % 2, 1].reshape(D, -1)
    column = jnp.zeros((1, w1.shape[1]), F32)
    for rows in blocks(n, step):
        f = (dot_nn(a2_ref[rows, :], w1) + bias).astype(BF16)
        dh = dot_nn(gf_ref[rows, :], w2)
        f2 = f * f
        th = jnp.tanh(f * (low(SQRT_2_PI) + low(SQRT_2_PI * 0.044715) * f2))
        half = low(0.5) + low(0.5) * th
        h = f * half
        slope = half + f * (low(0.5) - low(0.5) * th * th) * (
            low(SQRT_2_PI) + low(3 * SQRT_2_PI * 0.044715) * f2
        )
        df = (dh * slope.astype(F32)).astype(BF16)
        h_ref[rows, :] = h
        df_ref[rows, :] = df
        column += jnp.sum(df.astype(F32), 0, keepdims=True)
        feed_ref[rows, :] += dot_nt(h, w2)
        da2_ref[rows, :] += dot_nt(df, w1)
    sums_ref[pl.ds(8 + mine, 1), :] = column

    @pl.when(t == 1)
    def _():
        recv(last)
        start(last_core)

    @pl.when(t == 0)
    def _():
        late[0].wait()

    def weight_grad(left_ref, right_ref):
        value = dot_nn(left_ref[...], right_ref[...])
        return value.reshape(Z_DEV, Y_DEV, depth, value.shape[-1]).astype(BF16)

    grad1 = weight_grad(a2t_ref, df_ref)
    grad2 = weight_grad(gft_ref, h_ref)

    def put(ref):
        ref[0] = grad1
        ref[1] = grad2

    def reduced(ref):
        return lambda i, s, z: (
            ref[i, z].astype(F32) + land_ref[s, i, z].astype(F32)
        ).astype(BF16)

    @pl.when(t == 0)
    def _():
        put(stage_ref)
        start(core[0])

    @pl.when(t == 1)
    def _():
        put(near_ref)
        recv(core[0])

        @pl.loop(0, Z_DEV)
        def _(z):
            for i in range(2):
                near_ref[i, z] = reduced(near_ref)(i, 0, z)

        start(cross)

    @pl.when(t == 2)
    def _():
        for copy in core[0]:
            copy.wait_send()
        put(stage_ref)
        start(core[1])

    @pl.when(t == 3)
    def _():
        put(work_ref)
        late[1].wait()
        for i, rows in enumerate(blocks(n, step)):
            live = live_rows(i)
            h1 = h1_ref[rows, :]
            out_ref[rows, :] = (live * (h1 + (feed_ref[rows, :] + rows_ref[7:8, :]))).astype(BF16)
            xhat, r = norm_parts(h1)
            da2 = da2_ref[rows, :]
            sums_ref[1:2, :] += jnp.sum(da2 * xhat, 0, keepdims=True)
            sums_ref[6:7, :] += jnp.sum(da2, 0, keepdims=True)
            dg = da2 * rows_ref[1:2, :]
            dv = r * (
                dg
                - jnp.mean(dg, -1, keepdims=True)
                - xhat * jnp.mean(dg * xhat, -1, keepdims=True)
            )
            dh1 = gf_ref[rows, :].astype(F32) + dv
            dh1_ref[rows, :] = dh1
            gb = dh1.astype(BF16)
            gb_ref[rows, :] = gb
            gbt_ref[:, rows] = gb.T
            sums_ref[5:6, :] += jnp.sum(gb.astype(F32), 0, keepdims=True)
            for copy in puts[i]:
                copy.start()
        put_gbt.start()
        recv(core[1])

        @pl.loop(0, Z_DEV)
        def _(z):
            for i in range(2):
                work_ref[i, z] = reduced(work_ref)(i, 1, z)

        put_work.start()
        recv(cross)

        @pl.loop(0, Z_DEV)
        def _(z):
            for i in range(2):
                fold_ref[i, z] = (
                    near_ref[i, z, y].astype(F32) + cross_ref[i, z].astype(F32)
                ).astype(BF16)

        links.sent(*core[0])
        for copies in puts + [[put_gbt, put_work]]:
            for copy in copies:
                copy.wait()


def run_fused_feed_forward(lengths, cot, a2, a2t, h1, g1, g2, rows):
    n = cot.shape[1]
    groups, _, _, depth, hidden = g1.shape
    both = (2, Z_DEV, Y_DEV, depth, hidden)
    fold = (2, Z_DEV, depth, hidden)
    return pl.pallas_call(
        fused_feed_forward,
        grid=(groups,),
        in_specs=[SMEM_WHOLE, ANY_WHOLE, VMEM_WHOLE] + [ANY_WHOLE] * 4 + [VMEM_WHOLE],
        out_specs=[ANY_WHOLE, VMEM_WHOLE] + [ANY_WHOLE] * 4 + [VMEM_WHOLE],
        out_shape=[
            shaped(BF16, n, D), shaped(BF16, *fold), shaped(BF16, *both), shaped(F32, n, D),
            shaped(BF16, n, D), shaped(BF16, D, n), shaped(F32, 16, D),
        ],
        scratch_shapes=[
            pltpu.VMEM((n, D), BF16), pltpu.VMEM((D, n), BF16), pltpu.VMEM((n, D), F32),
            pltpu.VMEM((n, D), F32), pltpu.VMEM((n, hidden), BF16), pltpu.VMEM((n, hidden), BF16),
            pltpu.VMEM((2,) + both, BF16),
            pltpu.VMEM((2,) + fold, BF16), pltpu.VMEM(fold, BF16), pltpu.VMEM(both, BF16),
            pltpu.VMEM((2,) + both, BF16),
            pltpu.VMEM(both, BF16), pltpu.VMEM(fold, BF16),
            pltpu.VMEM((D, n), BF16), pltpu.VMEM((n, D), F32), pltpu.VMEM((n, D), BF16),
            pltpu.VMEM(both, BF16),
            pltpu.SemaphoreType.DMA((12,)), pltpu.SemaphoreType.DMA((12,)),
            pltpu.SemaphoreType.DMA((9,)), pltpu.SemaphoreType.DMA((3, n // 256)),
        ],
        compiler_params=pltpu.CompilerParams(
            vmem_limit_bytes=VMEM_LIMIT, collective_id=1, has_side_effects=True
        ),
        name="fused_feed_forward",
    )(lengths, cot, a2, a2t, h1, g1, g2, rows)
class Reduce:
    def __init__(
        self, links, place, work, acc, cross_ref, far_ref, mid_ref, last_ref, side_ref,
        slots=(0, 1),
    ):
        self.place, self.work, self.acc = place, work, acc
        self.cross_ref, self.far_ref, self.mid_ref = cross_ref, far_ref, mid_ref
        self.last_ref, self.side_ref = last_ref, side_ref
        zs = place.zs
        self.y = {
            s: [
                links.add(place.to_y, work(s, zs[j], place.other_y), cross_ref.at[s, zs[j]])
                for j in (1, 3, 2, 0)
            ]
            for s in slots
        }
        self.z = [
            [
                links.add(place.to_z[1], acc(s, zs[1]), far_ref.at[s, 0]),
                links.add(place.to_z[1], acc(s, zs[3]), far_ref.at[s, 1]),
                links.add(place.to_z[2], mid_ref.at[s, 1], far_ref.at[s, 2]),
            ]
            for s in range(2)
        ]
        self.x = links.add(place.to_x, last_ref, side_ref)

    def fold_y(self, s, half):
        for i, j in [(0, 1), (1, 3), (2, 2), (3, 0)][2 * half : 2 * half + 2]:
            z = self.place.zs[j]
            recv(self.y[s][i])
            value = self.work(s, z, self.place.y)[...].astype(F32)
            self.acc(s, z)[...] = (value + self.cross_ref[s, z].astype(F32)).astype(BF16)
            if i < 2:
                start(self.z[s][i])

    def fold_z(self, s):
        recv(self.z[s][:2])
        for i in (1, 0):
            value = self.acc(s, self.place.zs[2 * i])[...].astype(F32)
            self.mid_ref[s, i] = (value + self.far_ref[s, i].astype(F32)).astype(BF16)
            if i:
                start(self.z[s][2])

    def own(self, s):
        recv(self.z[s][2])
        return self.mid_ref[s, 0].astype(F32) + self.far_ref[s, 2].astype(F32)

    def send_x(self):
        self.last_ref[...] = self.own(1).astype(BF16)
        start(self.x)

    def total(self):
        value = self.own(0)
        recv(self.x)
        return value + self.side_ref[...].astype(F32)


def fused_backward(
    tokens_ref, gq_in, gw_in, rows_ref, dh1_ref, gb_ref, gbt_in, q_in, v_in, kt_in,
    p_ref, scale_in, o_in, a1t_in, layer_in, fold_in, work_in, early_ref,
    out_ref, layerout_ref, part0_ref, partw_ref, part1_ref, part2_ref, total_ref,
    gq_ref, gw_ref, q_ref, v_ref, kt_ref, scale_ref, o_ref,
    a1t_ref, gbt_ref, layer_ref, fold_ref, work_ref, do_ref, delta_ref, dkv_ref, dqkv_ref, da1_ref, own_ref, passing_ref, passlayer_ref, bqv_ref,
    folded_ref, cross1_ref, far1_ref, mid1_ref, last1_ref, side1_ref,
    cross2_ref, far2_ref, mid2_ref, last2_ref, side2_ref,
    stagew_ref, landw_ref, workw_ref, crossw_ref, farw_ref, midw_ref, lastw_ref, sidew_ref,
    stage0_ref, land0_ref, work0_ref, cross0_ref, far0_ref, mid0_ref, last0_ref, side0_ref,
    sums_ref, sumland_ref,
    send_sem, recv_sem, local_sem, result_sem, group_sem,
):
    t = pl.program_id(0)
    n = own_ref.shape[0]
    width = gw_ref.shape[-1]
    depth = part0_ref.shape[0]
    heads = width // HEAD_DIM
    step = n // 4
    place = Place()
    y = place.y
    links = Links(send_sem, recv_sem)
    k, i = group_and_block(t)
    mine = place.group(k)
    now = k % 2
    out = Result(links, place, own_ref, passing_ref, out_ref, step, result_sem.at[0])
    layer = Result(links, place, layer_ref, passlayer_ref, layerout_ref, step, result_sem.at[1])
    fetch = pltpu.make_async_copy(tokens_ref.at[place.t], own_ref, local_sem.at[0])
    fetch_layer, fetch_work, fetch_fold, fetch_gbt, fetch_a1t = [
        pltpu.make_async_copy(there, here, local_sem.at[1 + j])
        for j, (there, here) in enumerate([
            (layer_in, layer_ref), (work_in, work_ref), (fold_in, fold_ref),
            (gbt_in, gbt_ref), (a1t_in, a1t_ref),
        ])
    ]
    def operands(group):
        slot = group % 2
        pairs = [
            (gw_in, gw_ref), (scale_in, scale_ref), (o_in, o_ref), (v_in, v_ref),
            (q_in, q_ref), (kt_in, kt_ref), (gq_in, gq_ref),
        ]
        return [
            pltpu.make_async_copy(there.at[group], here.at[slot], group_sem.at[slot, j])
            for j, (there, here) in enumerate(pairs)
        ]

    corew = [links.add(place.to_core, stagew_ref, landw_ref.at[i]) for i in range(2)]
    core0 = [links.add(place.to_core, stage0_ref, land0_ref.at[i]) for i in range(2)]
    def half_done(i, *landing):
        return Reduce(
            links, place, lambda s, z, y: work_ref.at[i, z, y],
            lambda s, z: folded_ref.at[i, z] if s else fold_ref.at[i, z],
            *landing, slots=(1,),
        )

    seg1 = half_done(0, cross1_ref, far1_ref, mid1_ref, last1_ref, side1_ref)
    seg2 = half_done(1, cross2_ref, far2_ref, mid2_ref, last2_ref, side2_ref)
    segw = Reduce(
        links, place, lambda s, z, y: workw_ref.at[s, z, y],
        lambda s, z: workw_ref.at[s, z, y],
        crossw_ref, farw_ref, midw_ref, lastw_ref, sidew_ref,
    )
    seg0 = Reduce(
        links, place, lambda s, z, y: work0_ref.at[s, z, y],
        lambda s, z: work0_ref.at[s, z, y],
        cross0_ref, far0_ref, mid0_ref, last0_ref, side0_ref,
    )
    sum_core, sum_y, *sum_z, sum_x = [
        links.add(to, sums_ref.at[i], sumland_ref.at[j])
        for j, (i, to) in enumerate(
            zip([0, 1, 2, 2, 2, 3], [place.to_core, place.to_y] + place.to_z[1:] + [place.to_x])
        )
    ]

    def when(point):
        return pl.when(t == point)

    @when(0)
    def _():
        start(fetch_layer, operands(1), fetch_work, fetch_fold, fetch_gbt, operands(0))
        start(fetch, fetch_a1t)
        place.greet()
        fetch_layer.wait()
        for i in range(4):
            layer.send(i)
        fetch_work.wait()
        start(seg1.y[1], seg2.y[1])
        fetch_fold.wait()
        start(seg1.z[0][:2], seg2.z[0][:2])
        bqv_ref[...] = jnp.zeros_like(bqv_ref)
        sums_ref[0] = early_ref[...]
        da1_ref[...] = jnp.zeros_like(da1_ref)
        fetch_gbt.wait()

    def add_core():
        recv(corew[1])

        @pl.loop(0, Z_DEV)
        def _(z):
            workw_ref[1, z] = (
                workw_ref[1, z].astype(F32) + landw_ref[1, z].astype(F32)
            ).astype(BF16)

        start(segw.y[1])

    def wait(copies):
        for copy in copies:
            copy.wait()

    @when(0)
    def _():
        wait(operands(1))

    @when(4)
    def _():
        start(operands(3))
        wait(operands(0))

    @when(8)
    def _():
        start(operands(2))
        wait(operands(3))

    @when(9)
    def _():
        wait(operands(2))

    plan = [
        (2, 1, lambda: (seg1.fold_y(1, 0), seg1.fold_z(0))),
        (3, 1, lambda: layer.pass_on(0)),
        (4, 0, lambda: (seg1.fold_y(1, 1), seg2.fold_z(0))),
        (4, 1, lambda: layer.pass_on(1)),
        (5, 1, lambda: (seg1.fold_z(1), seg2.fold_y(1, 0))),
        (8, 0, lambda: (seg2.fold_y(1, 1), layer.pass_on(2))),
        (8, 1, lambda: (seg1.send_x(), segw.fold_y(0, 0), segw.fold_y(0, 1))),
        (9, 0, add_core),
        (9, 1, lambda: (seg2.fold_z(1), seg0.fold_y(0, 0), layer.pass_on(3))),
        (10, 1, lambda: segw.fold_z(0)),
        (11, 1, lambda: (seg2.send_x(), seg0.fold_y(0, 1))),
        (12, 1, lambda: (segw.fold_y(1, 0), segw.fold_y(1, 1))),
        (13, 1, lambda: (seg0.fold_z(0), out.pass_on(3))),
        (14, 1, lambda: segw.fold_z(1)),
    ]

    def serve(point):
        for at, where, act in plan:
            if where == point:
                pl.when(t == at)(lambda act=act: (act(), None)[1])

    @pl.when((t == 0) | (t == 4) | (t == 8) | (t == 9))
    def _():
        pick = (
            lax.broadcasted_iota(jnp.int32, (8, width), 1) // HEAD_DIM
            == lax.broadcasted_iota(jnp.int32, (8, width), 0)
        ).astype(BF16)

        @pl.loop(0, n // step)
        def _(i):
            rows = pl.ds(pl.multiple_of(i * step, step), step)
            columns = scale_ref[now, :, rows].T
            lane = lax.broadcasted_iota(jnp.int32, (step, width), 1)
            scale = columns[:, heads - 1 : heads]
            for h in reversed(range(heads - 1)):
                scale = jnp.where(lane < (h + 1) * HEAD_DIM, columns[:, h : h + 1], scale)
            do = (dot_nn(gb_ref[rows, :], gw_ref[now]) * scale).astype(BF16)
            do_ref[now, rows, :] = do
            product = do.astype(F32) * o_ref[now, rows, :].astype(F32)
            high = product.astype(BF16)
            low = (product - high.astype(F32)).astype(BF16)
            delta_ref[now, :, rows] = dot_nt(pick, high) + dot_nt(pick, low)

        value = dot_nn(gbt_ref[...], o_ref[now]).reshape(Z_DEV, Y_DEV, depth, width)
        for s in range(2):
            @when(8 * s)
            def _():
                if s:
                    corew[0].wait_send()
                stagew_ref[...] = value.astype(BF16)
                start(corew[s])

        @when(4)
        def _():
            recv(corew[0])
            workw_ref[0] = (value + landw_ref[0].astype(F32)).astype(BF16)
            start(segw.y[0])

        @when(9)
        def _():
            workw_ref[1] = value.astype(BF16)

    serve(0)

    for ii in reversed(range(4)):
        @pl.when(i == ii)
        def _():
            first, last = ii * step, (ii + 1) * step
            do = do_ref[now, first:last, :]
            q = q_ref[now, first:last, :]
            v = v_ref[now, :last, :]
            lane = lax.broadcasted_iota(jnp.int32, (1, width), 1)
            dk, dv, dq = None, None, []
            for h in range(heads):
                low, high = h * HEAD_DIM, (h + 1) * HEAD_DIM
                here = (lane >= low) & (lane < high)
                p = p_ref[0, h, :last, :]
                dp = dot_nt(v, jnp.where(here, do, jnp.zeros((), BF16)))
                ds = p * (dp - delta_ref[now, h : h + 1, first:last]).astype(BF16)
                part = dot_nn(p, do)
                dv = part if dv is None else jnp.where(lane < low, dv, part)
                part = dot_nn(ds, q)
                dk = part if dk is None else jnp.where(lane < low, dk, part)
                dq.append(dot_nn(kt_ref[now, low:high, :last], ds))
            if ii == 3:
                dkv_ref[now, 0] = dk
                dkv_ref[now, 1] = dv
            else:
                dkv_ref[now, 0, :last, :] += dk
                dkv_ref[now, 1, :last, :] += dv
            dk = dkv_ref[now, 0, first:last, :].astype(BF16)
            dv = dkv_ref[now, 1, first:last, :].astype(BF16)
            dq = (jnp.concatenate(dq, 0) * HEAD_DIM ** -0.5).astype(BF16).T
            dqkv_ref[now, first:last, :width] = dq
            dqkv_ref[now, first:last, width : 2 * width] = dk
            dqkv_ref[now, first:last, 2 * width :] = dv
            bqv_ref[mine, 0:1, :] += jnp.sum(dq.astype(F32), 0, keepdims=True)
            bqv_ref[mine, 1:2, :] += jnp.sum(dv.astype(F32), 0, keepdims=True)
            da1_ref[first:last, :] += dot_nt(dqkv_ref[now, first:last, :], gq_ref[now])

    serve(1)

    @pl.when((t > 8) & (t % 2 == 1))
    def _():
        rows = pl.ds(pl.multiple_of(i * step, step), step)
        xhat, r = norm_parts(own_ref[rows, :].astype(F32))
        da1 = da1_ref[rows, :]
        sums_ref[0, 0:1, :] += jnp.sum(da1 * xhat, 0, keepdims=True)
        sums_ref[0, 2:3, :] += jnp.sum(da1, 0, keepdims=True)
        dg = da1 * rows_ref[0:1, :]
        dv = r * (
            dg
            - jnp.mean(dg, -1, keepdims=True)
            - xhat * jnp.mean(dg * xhat, -1, keepdims=True)
        )
        own_ref[rows, :] = (dh1_ref[...] + dv).astype(BF16)
        for ii in range(4):
            @pl.when(i == ii)
            def _():
                out.send(ii)

    @pl.when((t == 3) | (t == 7) | (t > 13))
    def _():
        @when(3)
        def _():
            fetch.wait()
            fetch_a1t.wait()

        value = dot_nn(a1t_ref[...], dqkv_ref[now]).reshape(Z_DEV, Y_DEV, depth, 3 * width)
        for s in range(2):
            @when(3 + 11 * s)
            def _():
                if s:
                    core0[0].wait_send()
                stage0_ref[...] = value.astype(BF16)
                start(core0[s])

            @when(7 + 8 * s)
            def _():
                recv(core0[s])
                work0_ref[s] = (value + land0_ref[s].astype(F32)).astype(BF16)
                start(seg0.y[s])

    @when(15)
    def _():
        for s in range(4):
            sums_ref[0, 3:5, s * width : (s + 1) * width] = bqv_ref[s, 0:2, :]
        start(sum_core)
        segw.send_x()
        out.pass_on(2)
        recv(sum_core)
        sums_ref[1] = sums_ref[0] + sumland_ref[0]
        start(sum_y)
        seg0.fold_y(1, 0)
        out.pass_on(1)
        seg0.fold_y(1, 1)
        recv(sum_y)
        sums_ref[2] = sums_ref[1] + sumland_ref[1]
        start(sum_z)
        seg0.fold_z(1)
        recv(sum_z)
        sums_ref[3] = (sums_ref[2] + sumland_ref[2]) + (sumland_ref[3] + sumland_ref[4])
        start(sum_x)
        part1_ref[...] = seg1.total()
        part2_ref[...] = seg2.total()
        seg0.send_x()
        partw_ref[...] = segw.total()
        layer.finish()
        out.pass_on(0)
        recv(sum_x)
        total_ref[...] = sums_ref[3] + sumland_ref[5]
        part0_ref[...] = seg0.total()
        out.finish()
        links.sent(corew[0], core0[0])


def group_and_block(t):
    early = t < 8
    return (
        jnp.where(early, 1 - t // 4, 3 - t % 2),
        3 - jnp.where(early, t % 4, jnp.maximum(t - 8, 0) // 2),
    )


def run_fused_backward(
    tokens, gq, gw, rows, dh1, gb, gbt, q, v, kt, p, scale, o, a1t, layer, fold, work, early
):
    groups, n, _ = tokens.shape
    width = gw.shape[-1]
    heads = width // HEAD_DIM
    hidden = fold.shape[-1]
    depth = D // (Z_DEV * Y_DEV)
    step = n // 4

    p_spec = pl.BlockSpec(
        (1, heads, n, step),
        lambda t: (group_and_block(t)[0], 0, 0, group_and_block(t)[1]),
    )

    copies = 2 * 12 + 4 + 2 * 15 + 2 * 11 + 6

    def landing(lanes):
        return [
            pltpu.VMEM((2, Z_DEV, depth, lanes), BF16),
            pltpu.VMEM((2, 3, depth, lanes), BF16), pltpu.VMEM((2, 2, depth, lanes), BF16),
            pltpu.VMEM((depth, lanes), BF16), pltpu.VMEM((depth, lanes), BF16),
        ]

    def working(lanes):
        block = (Z_DEV, Y_DEV, depth, lanes)
        return [pltpu.VMEM(block, BF16)] + [pltpu.VMEM((2,) + block, BF16)] * 2

    return pl.pallas_call(
        fused_backward,
        grid=(4 * groups,),
        in_specs=[
            ANY_WHOLE, ANY_WHOLE, ANY_WHOLE, VMEM_WHOLE,
            pl.BlockSpec((step, D), lambda t: (group_and_block(jnp.maximum(t, 8))[1], 0)),
            VMEM_WHOLE, ANY_WHOLE, ANY_WHOLE, ANY_WHOLE, ANY_WHOLE, p_spec,
            ANY_WHOLE, ANY_WHOLE, ANY_WHOLE, ANY_WHOLE, ANY_WHOLE, ANY_WHOLE, VMEM_WHOLE,
        ],
        out_specs=[ANY_WHOLE] * 2 + [VMEM_WHOLE] * 5,
        out_shape=[
            shaped(BF16, groups, n, D), shaped(BF16, groups, n, D),
            shaped(F32, depth, 3 * width),
            shaped(F32, depth, width), shaped(F32, depth, hidden),
            shaped(F32, depth, hidden), shaped(F32, 16, D),
        ],
        scratch_shapes=[
            pltpu.VMEM((2, D, 3 * width), BF16), pltpu.VMEM((2, D, width), BF16),
            pltpu.VMEM((2, n, width), BF16), pltpu.VMEM((2, n, width), BF16),
            pltpu.VMEM((2, width, n), BF16), pltpu.VMEM((2, 8, n), F32),
            pltpu.VMEM((2, n, width), BF16),
            pltpu.VMEM((D, n), BF16), pltpu.VMEM((D, n), BF16), pltpu.VMEM((n, D), BF16),
            pltpu.VMEM((2, Z_DEV, depth, hidden), BF16),
            pltpu.VMEM((2, Z_DEV, Y_DEV, depth, hidden), BF16),
            pltpu.VMEM((2, n, width), BF16),
            pltpu.VMEM((2, 8, n), F32), pltpu.VMEM((2, 2, n, width), F32),
            pltpu.VMEM((2, n, 3 * width), BF16), pltpu.VMEM((n, D), F32),
            pltpu.VMEM((n, D), BF16), pltpu.VMEM((n, D), BF16), pltpu.VMEM((n, D), BF16),
            pltpu.VMEM((groups, 8, width), F32),
        ]
        + landing(hidden)[:1] + landing(hidden) + landing(hidden)
        + working(width) + landing(width)
        + working(3 * width) + landing(3 * width)
        + [
            pltpu.VMEM((4, 16, D), F32), pltpu.VMEM((6, 16, D), F32),
            pltpu.SemaphoreType.DMA((copies,)), pltpu.SemaphoreType.DMA((copies,)),
            pltpu.SemaphoreType.DMA((6,)), pltpu.SemaphoreType.DMA((2, 2, 4)),
            pltpu.SemaphoreType.DMA((2, 7)),
        ],
        compiler_params=pltpu.CompilerParams(
            vmem_limit_bytes=VMEM_LIMIT, collective_id=2, has_side_effects=True
        ),
        name="fused_backward",
    )(tokens, gq, gw, rows, dh1, gb, gbt, q, v, kt, p, scale, o, a1t, layer, fold, work, early)


def place_gradients(
    tie_ref, sums_ref, part0_ref, partw_ref, part1_ref, part2_ref, near_out_ref,
    near_grad_ref, far_out_ref, far_grad_ref, gains_ref, bias_ref, in_ref, out_ref, expand_ref,
    project_ref,
):
    far_out_ref[...] = near_out_ref[...]
    far_grad_ref[...] = near_grad_ref[...]
    own = gains_ref.shape[-1]
    width = partw_ref.shape[-1]

    @pl.when(pl.program_id(0) == 0)
    def _():
        first = (lax.axis_index("dp") * 4 + lax.axis_index("tensor")) * own
        feature = lax.broadcasted_iota(jnp.int32, (D, 128), 0)
        lane = lax.broadcasted_iota(jnp.int32, (D, 128), 1)
        chosen = ((feature == first + lane) & (lane < own)).astype(F32)
        sums = lax.dot_general(
            sums_ref[...], chosen, (((1,), (0,)), ((), ())),
            precision=lax.Precision.HIGHEST, preferred_element_type=F32,
        )[:, :own]
        s0, s1, s2, s3 = tie_ref[0], tie_ref[1], tie_ref[2], tie_ref[3]
        w_out = partw_ref[...].T

        def at(source, wanted, value):
            return jnp.where(source == wanted, value, jnp.zeros_like(value))

        row = lax.broadcasted_iota(jnp.int32, (NSRC, own), 0)
        for i, wanted in enumerate([s0, s0, s0, s1, s2, s3, s2, s2, s2, s2]):
            bias_ref[i] = jnp.where(row == wanted, sums[2 + i : 3 + i], 0.0)
        for s in range(NSRC):
            gains_ref[s, 0:1] = at(s, s0, sums[0:1])
            gains_ref[s, 1:2] = at(s, s2, sums[1:2])
            for j in range(3):
                in_ref[s, j] = at(s, s0, part0_ref[:, j * width : (j + 1) * width])
            out_ref[s] = at(s, s1, w_out)
            expand_ref[s] = at(s, s2, part1_ref[...])
            project_ref[s] = at(s, s3, part2_ref[...])


def run_place_gradients(tie, sums, part0, partw, part1, part2, out, grad, like):
    slots, n, _ = grad.shape
    gains, biases, w_in, w_out, w_expand, w_project = [item.shape for item in like]
    shapes = [
        gains, (biases[1], biases[0], biases[2]), w_in, w_out, w_expand,
        (w_project[0], w_project[2], w_project[1]),
    ]
    out, grad, gains, biases, w_in, w_out, w_expand, w_project = pl.pallas_call(
        place_gradients,
        grid=(slots,),
        in_specs=[SMEM_WHOLE] + [VMEM_WHOLE] * 5
        + [group(n, D), group(n, D)],
        out_specs=[group(n, D), group(n, D)] + [VMEM_WHOLE] * 6,
        out_shape=[shaped(BF16, slots, n, D)] * 2 + [shaped(F32, *item) for item in shapes],
        compiler_params=pltpu.CompilerParams(vmem_limit_bytes=VMEM_LIMIT),
        name="place_gradients",
    )(tie, sums, part0, partw, part1, part2, out, grad)
    biases = biases.transpose(1, 0, 2)
    return out, grad, gains, biases, w_in, w_out, w_expand, w_project.transpose(0, 2, 1)


def plain_step(
    tokens, lengths, tie_map, norm_gains, bias_rows, attention_in, attention_out,
    expand_weight, project_weight, cotangent,
):
    slot_rows = tokens.shape[0] // lengths.shape[0]
    me = lax.axis_index("tensor")
    in_local = lax.dynamic_index_in_dim(attention_in, tie_map[0], 0, keepdims=False)
    out_local = lax.dynamic_index_in_dim(attention_out, tie_map[1], 0, keepdims=False)
    expand_local = lax.dynamic_index_in_dim(expand_weight, tie_map[2], 0, keepdims=False)
    project_local = lax.dynamic_index_in_dim(project_weight, tie_map[3], 0, keepdims=False)
    local0 = jnp.concatenate([in_local, out_local.T[None]], 0)
    row_kinds = jnp.array([0, 0, 0, 1, 2, 3] + [2] * (FF // D), dtype=jnp.int32)
    gain_kinds = jnp.array([0, 2], dtype=jnp.int32)
    gain_pick = norm_gains[tie_map[gain_kinds], jnp.arange(2)]
    bias_pick = bias_rows[tie_map[row_kinds], jnp.arange(row_kinds.shape[0])]
    vectors = jnp.concatenate([gain_pick, bias_pick], 0)
    x = lax.dynamic_slice_in_dim(tokens, me * slot_rows, slot_rows, 0)
    cot = lax.dynamic_slice_in_dim(cotangent, me * slot_rows, slot_rows, 0)
    length = lax.dynamic_slice_in_dim(lengths, me, 1, 0)
    rows = lax.all_gather(vectors, ("dp", "tensor"), axis=1, tiled=True).astype(F32)
    rows = jnp.concatenate([rows, jnp.zeros((4, D), F32)], 0)

    def gathered(piece, axis):
        piece = lax.all_gather(piece, "dp", axis=axis, tiled=True)
        return lax.all_gather(piece, "tensor", axis=0)

    g0 = gathered(local0, 1)
    g1 = gathered(expand_local, 0)
    g2 = gathered(project_local.T, 0)
    groups, width = g0.shape[0], g0.shape[-1]
    bqv = rows[3:5].reshape(2, groups, width).transpose(1, 0, 2)
    q, v, kt, p, o, a1t, h1, a2, a2t = run_attention_forward(length, x, g0, rows, bqv)
    out, d1, d2, dh1, gb, gbt, sums = run_feed_forward(length, cot, a2, a2t, h1, g1, g2, rows)
    d0, xg, sums_in, sums_qv = run_attention_backward(
        x, g0, rows, dh1, gb, gbt, q, v, kt, p, o, a1t
    )
    layer_out = lax.all_gather(out, "tensor", axis=0, tiled=True)
    tokens_grad = lax.all_gather(xg, "tensor", axis=0, tiled=True)

    def scattered(piece, axis):
        piece = lax.psum_scatter(piece, "tensor", scatter_dimension=0)
        return lax.psum_scatter(piece, "dp", scatter_dimension=axis, tiled=True).astype(F32)

    part0 = scattered(d0, 1)
    part1 = scattered(d1, 0)
    part2 = scattered(d2, 0)
    qv = sums_qv[:, :2].transpose(1, 0, 2).reshape(2, D)
    sums = jnp.concatenate(
        [sums_in[0:1], sums[1:2], sums_in[1:2], qv, sums[5:12]], 0
    )
    sums = lax.psum_scatter(sums, ("dp", "tensor"), scatter_dimension=1, tiled=True)
    return layer_out, tokens_grad, *placed(tie_map, sums, part0, part1, part2)


def fused_step(
    tokens, lengths, tie_map, norm_gains, bias_rows, attention_in, attention_out,
    expand_weight, project_weight, cotangent,
):
    slots = lengths.shape[0]
    tokens = tokens.reshape(slots, -1, D)
    cotangent = cotangent.reshape(slots, -1, D)
    gq, gw, g1, g2, rows, q, v, kt, p, scale, o, a1t, h1, a2, a2t = run_fused_forward(
        tie_map, lengths, tokens, norm_gains, bias_rows, attention_in, attention_out,
        expand_weight, project_weight,
    )
    layer, fold, work, dh1, gb, gbt, early = run_fused_feed_forward(
        lengths, cotangent, a2, a2t, h1, g1, g2, rows
    )
    grad, out, part0, partw, part1, part2, sums = run_fused_backward(
        tokens, gq, gw, rows, dh1, gb, gbt, q, v, kt, p, scale, o, a1t, layer, fold,
        work, early,
    )
    out, grad, *placed_grads = run_place_gradients(
        tie_map, sums, part0, partw, part1, part2, out, grad,
        (norm_gains, bias_rows, attention_in, attention_out, expand_weight, project_weight),
    )
    return out.reshape(-1, D), grad.reshape(-1, D), *placed_grads


def placed(tie_map, sums, part0, part1, part2):
    source = jnp.arange(NSRC, dtype=jnp.int32)

    def place(piece, which):
        pick = (source == tie_map[which]).reshape((NSRC,) + (1,) * piece.ndim)
        return jnp.where(pick, piece[None], 0.0)

    def place_rows(piece, kinds):
        pick = source[:, None] == tie_map[jnp.array(kinds, dtype=jnp.int32)][None, :]
        return jnp.where(pick[:, :, None], piece[None], 0.0)

    return (
        place_rows(sums[:2], [0, 2]),
        place_rows(sums[2:], [0, 0, 0, 1, 2, 3] + [2] * (FF // D)),
        place(part0[:3], 0),
        place(part0[3].T, 1),
        place(part1, 2),
        place(part2.T, 3),
    )


def solution(mesh):
    fused = mesh.shape["dp"] == Z_DEV * Y_DEV and mesh.shape["tensor"] == X_DEV * C_DEV
    return jax.shard_map(
        fused_step if fused else plain_step,
        mesh=mesh,
        in_specs=(
            P("dp", None),
            P("dp"),
            P(),
            P(None, None, ("dp", "tensor")),
            P(None, None, ("dp", "tensor")),
            P(None, None, "dp", "tensor"),
            P(None, "tensor", "dp"),
            P(None, "dp", "tensor"),
            P(None, "tensor", "dp"),
            P("dp", None),
        ),
        out_specs=(
            P("dp", None),
            P("dp", None),
            P(None, None, ("dp", "tensor")),
            P(None, None, ("dp", "tensor")),
            P(None, None, "dp", "tensor"),
            P(None, "tensor", "dp"),
            P(None, "dp", "tensor"),
            P(None, "tensor", "dp"),
        ),
        check_vma=False,
    )
```

```python
import jax
import jax.numpy as jnp
from jax import lax
from jax.experimental import pallas as pl
from jax.experimental.pallas import tpu as pltpu
from jax.sharding import PartitionSpec as P

D = 768
HEAD_DIM = 64
FF = 3072
NSRC = 4
EPS = 1e-05
MASKED = -1e30
F32 = jnp.float32
BF16 = jnp.bfloat16
VMEM_LIMIT = 60 * 1024 * 1024


def dot_nn(a, b):
    return lax.dot_general(a, b, (((1,), (0,)), ((), ())), preferred_element_type=F32)


def dot_nt(a, b):
    return lax.dot_general(a, b, (((1,), (1,)), ((), ())), preferred_element_type=F32)


def norm_parts(v):
    center = jnp.mean(v, -1, keepdims=True)
    centered = v - center
    r = lax.rsqrt(jnp.mean(centered * centered, -1, keepdims=True) + EPS)
    return centered * r, r


def head_mask(shape, h):
    lane = lax.broadcasted_iota(jnp.int32, shape, 1)
    return (lane >= h * HEAD_DIM) & (lane < (h + 1) * HEAD_DIM)


def blocks(total, size):
    return [slice(i * size, (i + 1) * size) for i in range(total // size)]


def attention_forward(
    len_ref, x_ref, g_ref, rows_ref, bqv_ref,
    q_ref, v_ref, kt_ref, p_ref, o_ref, a1t_ref, h1_ref, a2_ref, a2t_ref,
    a1_ref, k_ref, vt_ref, ot_ref, attn_ref,
):
    t = pl.program_id(0)
    n = x_ref.shape[0]
    width = g_ref.shape[-1]
    heads = width // HEAD_DIM
    step = 256
    length = len_ref[0]

    @pl.when(t == 0)
    def _():
        @pl.loop(0, n // step)
        def _(b):
            rows = pl.ds(pl.multiple_of(b * step, step), step)
            xhat, _ = norm_parts(x_ref[rows, :].astype(F32))
            a1 = xhat * rows_ref[0:1, :] + rows_ref[2:3, :]
            a1_ref[rows, :] = a1.astype(BF16)
            a1t_ref[:, rows] = a1.astype(BF16).T
            attn_ref[rows, :] = x_ref[rows, :].astype(F32) + rows_ref[5:6, :]

    @pl.loop(0, n // step)
    def _(b):
        rows = pl.ds(pl.multiple_of(b * step, step), step)
        a1 = a1_ref[rows, :]
        q = (dot_nn(a1, g_ref[0, 0]) + bqv_ref[0, 0:1, :]).astype(BF16)
        q_ref[0, rows, :] = q * jnp.asarray(HEAD_DIM ** -0.5, BF16)
        k = dot_nn(a1, g_ref[0, 1]).astype(BF16)
        k_ref[rows, :] = k
        kt_ref[0, :, rows] = k.T
        v = (dot_nn(a1, g_ref[0, 2]) + bqv_ref[0, 1:2, :]).astype(BF16)
        v_ref[0, rows, :] = v
        vt_ref[:, rows] = v.T

    for h in range(heads):
        k = k_ref[...]
        k = jnp.where(head_mask(k.shape, h), k, jnp.zeros_like(k))
        for b in range(n // step):
            first, last = b * step, (b + 1) * step
            q = q_ref[0, first:last, :]
            key = lax.broadcasted_iota(jnp.int32, (last, step), 0)
            query = lax.broadcasted_iota(jnp.int32, (step, step), 1) + first
            s = dot_nt(k[:last], q)
            near = jnp.where(
                (key[first:] <= query) & (key[first:] < length), s[first:], MASKED
            )
            if b:
                far = jnp.where(key[:first] < length, s[:first], MASKED)
                top = jnp.maximum(
                    jnp.max(far, 0, keepdims=True), jnp.max(near, 0, keepdims=True)
                )
                e_far = jnp.exp(far - top)
                e_near = jnp.exp(near - top)
                total = jnp.sum(e_far, 0, keepdims=True) + jnp.sum(e_near, 0, keepdims=True)
                scale = 1.0 / total
                p_ref[0, h, :first, first:last] = (e_far * scale).astype(BF16)
            else:
                top = jnp.max(near, 0, keepdims=True)
                e_near = jnp.exp(near - top)
                scale = 1.0 / jnp.sum(e_near, 0, keepdims=True)
            p_ref[0, h, first:last, first:last] = (e_near * scale).astype(BF16)
            ot_ref[h * HEAD_DIM : (h + 1) * HEAD_DIM, first:last] = dot_nn(
                vt_ref[h * HEAD_DIM : (h + 1) * HEAD_DIM, :last],
                p_ref[0, h, :last, first:last],
            ).astype(BF16)

    @pl.loop(0, n // step)
    def _(b):
        rows = pl.ds(pl.multiple_of(b * step, step), step)
        o = ot_ref[:, rows].T
        o_ref[0, rows, :] = o
        attn_ref[rows, :] += dot_nt(o, g_ref[0, 3])

    @pl.when(t == pl.num_programs(0) - 1)
    def _():
        @pl.loop(0, n // step)
        def _(b):
            rows = pl.ds(pl.multiple_of(b * step, step), step)
            h1 = attn_ref[rows, :]
            h1_ref[rows, :] = h1
            xhat, _ = norm_parts(h1)
            a2 = (xhat * rows_ref[1:2, :] + rows_ref[6:7, :]).astype(BF16)
            a2_ref[rows, :] = a2
            a2t_ref[:, rows] = a2.T


SQRT_2_PI = 0.7978845608028654


def feed_forward_both(
    len_ref, c_ref, a2_ref, a2t_ref, h1_ref, w1_ref, w2_ref, rows_ref,
    out_ref, d1_ref, d2_ref, dh1_ref, gb_ref, gbt_ref, sums_ref,
    gf_ref, gft_ref, feed_ref, da2_ref, h_ref, df_ref,
):
    t = pl.program_id(0)
    n = c_ref.shape[0]
    step = 256
    length = len_ref[0]

    @pl.when(t == 0)
    def _():
        sums_ref[...] = jnp.zeros_like(sums_ref)

        @pl.loop(0, n // step)
        def _(b):
            rows = pl.ds(pl.multiple_of(b * step, step), step)
            place = b * step + lax.broadcasted_iota(jnp.int32, (step, 1), 0)
            live = (place < length).astype(F32)
            g = (c_ref[rows, :].astype(F32) * live).astype(BF16)
            gf_ref[rows, :] = g
            gft_ref[:, rows] = g.T
            sums_ref[7:8, :] += jnp.sum(g.astype(F32), 0, keepdims=True)

    bias = rows_ref[pl.ds(8 + t, 1), :]

    @pl.loop(0, n // step)
    def _(b):
        rows = pl.ds(pl.multiple_of(b * step, step), step)
        f = dot_nn(a2_ref[rows, :], w1_ref[0]) + bias
        dh = dot_nn(gf_ref[rows, :], w2_ref[0])
        f2 = f * f
        th = jnp.tanh(f * (SQRT_2_PI + (SQRT_2_PI * 0.044715) * f2))
        half = 0.5 + 0.5 * th
        h = (f * half).astype(BF16)
        slope = half + f * (0.5 - 0.5 * th * th) * (
            SQRT_2_PI + (3 * SQRT_2_PI * 0.044715) * f2
        )
        df = (dh * slope).astype(BF16)
        h_ref[rows, :] = h
        df_ref[rows, :] = df
        sums_ref[pl.ds(8 + t, 1), :] += jnp.sum(df.astype(F32), 0, keepdims=True)
        feed = dot_nt(h, w2_ref[0])
        da2 = dot_nt(df, w1_ref[0])

        @pl.when(t == 0)
        def _():
            feed_ref[rows, :] = feed
            da2_ref[rows, :] = da2

        @pl.when(t > 0)
        def _():
            feed_ref[rows, :] += feed
            da2_ref[rows, :] += da2

    @pl.loop(0, D // step)
    def _(b):
        rows = pl.ds(pl.multiple_of(b * step, step), step)
        d1_ref[0, rows, :] = dot_nn(a2t_ref[rows, :], df_ref[...]).astype(BF16)
        d2_ref[0, rows, :] = dot_nn(gft_ref[rows, :], h_ref[...]).astype(BF16)

    @pl.when(t == pl.num_programs(0) - 1)
    def _():
        @pl.loop(0, n // step)
        def _(b):
            rows = pl.ds(pl.multiple_of(b * step, step), step)
            place = b * step + lax.broadcasted_iota(jnp.int32, (step, 1), 0)
            live = (place < length).astype(F32)
            h1 = h1_ref[rows, :]
            out_ref[rows, :] = (live * (h1 + (feed_ref[rows, :] + rows_ref[7:8, :]))).astype(BF16)
            xhat, r = norm_parts(h1)
            da2 = da2_ref[rows, :]
            sums_ref[1:2, :] += jnp.sum(da2 * xhat, 0, keepdims=True)
            sums_ref[6:7, :] += jnp.sum(da2, 0, keepdims=True)
            dg = da2 * rows_ref[1:2, :]
            dv = r * (
                dg
                - jnp.mean(dg, -1, keepdims=True)
                - xhat * jnp.mean(dg * xhat, -1, keepdims=True)
            )
            dh1 = live * c_ref[rows, :].astype(F32) + dv
            dh1_ref[rows, :] = dh1
            gb = dh1.astype(BF16)
            gb_ref[rows, :] = gb
            gbt_ref[:, rows] = gb.T
            sums_ref[5:6, :] += jnp.sum(gb.astype(F32), 0, keepdims=True)


def attention_backward(
    x_ref, g_ref, rows_ref, dh1_ref, gb_ref, gbt_ref, q_ref, v_ref, kt_ref, p_ref,
    o_ref, a1t_ref,
    d0_ref, xg_ref, sums_ref, bqv_ref,
    do_ref, delta_ref, dqt_ref, dq_ref, dk_ref, dv_ref, da1_ref,
):
    t = pl.program_id(0)
    n = x_ref.shape[0]
    width = g_ref.shape[-1]
    heads = width // HEAD_DIM
    step = 256
    pick = (
        lax.broadcasted_iota(jnp.int32, (16, width), 1) // HEAD_DIM
        == lax.broadcasted_iota(jnp.int32, (16, width), 0)
    ).astype(BF16)

    @pl.loop(0, n // step)
    def _(b):
        rows = pl.ds(pl.multiple_of(b * step, step), step)
        do = dot_nn(gb_ref[rows, :], g_ref[0, 3]).astype(BF16)
        do_ref[rows, :] = do
        prod = do.astype(F32) * o_ref[0, rows, :].astype(F32)
        high = prod.astype(BF16)
        low = (prod - high.astype(F32)).astype(BF16)
        delta_ref[:, rows] = dot_nt(pick, high) + dot_nt(pick, low)

    dqt_ref[...] = jnp.zeros_like(dqt_ref)
    for b in range(n // step):
        first, last = b * step, (b + 1) * step
        do = do_ref[first:, :]
        q = q_ref[0, first:, :]
        v = v_ref[0, first:last, :]
        dk, dv = None, None
        for h in range(heads):
            mine = head_mask((1, width), h)
            zero = jnp.zeros((), BF16)
            p = p_ref[0, h, first:last, first:]
            dp = dot_nt(jnp.where(mine, v, zero), do)
            ds = (p.astype(F32) * (dp - delta_ref[h : h + 1, first:])).astype(BF16)
            part = dot_nn(p, jnp.where(mine, do, zero))
            dv = part if dv is None else dv + part
            part = dot_nn(ds, jnp.where(mine, q, zero))
            dk = part if dk is None else dk + part
            head = slice(h * HEAD_DIM, (h + 1) * HEAD_DIM)
            dqt_ref[head, first:] += dot_nn(kt_ref[0, head, first:last], ds)
        dk_ref[first:last, :] = dk.astype(BF16)
        dv_ref[first:last, :] = dv.astype(BF16)

    @pl.when(t == 0)
    def _():
        da1_ref[...] = jnp.zeros_like(da1_ref)

    bqv_ref[...] = jnp.zeros_like(bqv_ref)

    @pl.loop(0, n // step)
    def _(b):
        rows = pl.ds(pl.multiple_of(b * step, step), step)
        dq = (dqt_ref[:, rows] * HEAD_DIM ** -0.5).astype(BF16).T
        dk = dk_ref[rows, :]
        dv = dv_ref[rows, :]
        dq_ref[rows, :] = dq
        bqv_ref[0, 0:1, :] += jnp.sum(dq.astype(F32), 0, keepdims=True)
        bqv_ref[0, 1:2, :] += jnp.sum(dv.astype(F32), 0, keepdims=True)
        da1_ref[rows, :] += (
            dot_nt(dq, g_ref[0, 0]) + dot_nt(dk, g_ref[0, 1]) + dot_nt(dv, g_ref[0, 2])
        )

    @pl.loop(0, D // step)
    def _(b):
        rows = pl.ds(pl.multiple_of(b * step, step), step)
        a1t = a1t_ref[rows, :]
        d0_ref[0, 0, rows, :] = dot_nn(a1t, dq_ref[...]).astype(BF16)
        d0_ref[0, 1, rows, :] = dot_nn(a1t, dk_ref[...]).astype(BF16)
        d0_ref[0, 2, rows, :] = dot_nn(a1t, dv_ref[...]).astype(BF16)
        d0_ref[0, 3, rows, :] = dot_nn(gbt_ref[rows, :], o_ref[0]).astype(BF16)

    @pl.when(t == pl.num_programs(0) - 1)
    def _():
        sums_ref[...] = jnp.zeros_like(sums_ref)

        @pl.loop(0, n // step)
        def _(b):
            rows = pl.ds(pl.multiple_of(b * step, step), step)
            xhat, r = norm_parts(x_ref[rows, :].astype(F32))
            da1 = da1_ref[rows, :]
            sums_ref[0:1, :] += jnp.sum(da1 * xhat, 0, keepdims=True)
            sums_ref[1:2, :] += jnp.sum(da1, 0, keepdims=True)
            dg = da1 * rows_ref[0:1, :]
            dv = r * (
                dg
                - jnp.mean(dg, -1, keepdims=True)
                - xhat * jnp.mean(dg * xhat, -1, keepdims=True)
            )
            xg_ref[rows, :] = (dh1_ref[rows, :] + dv).astype(BF16)


def whole(*shape):
    return pl.BlockSpec(shape, lambda t: (0,) * len(shape))


def group(*shape):
    return pl.BlockSpec((1,) + shape, lambda t: (t,) + (0,) * len(shape))


def shaped(dtype, *shape):
    return jax.ShapeDtypeStruct(shape, dtype)


SMEM_WHOLE = pl.BlockSpec(memory_space=pltpu.SMEM)


def run_attention_forward(length, x, g0, rows, bqv):
    n = x.shape[0]
    groups, _, _, width = g0.shape
    heads = width // HEAD_DIM
    return pl.pallas_call(
        attention_forward,
        grid=(groups,),
        in_specs=[SMEM_WHOLE, whole(n, D), group(4, D, width), whole(16, D), group(2, width)],
        out_specs=[
            group(n, width), group(n, width), group(width, n), group(heads, n, n),
            group(n, width), whole(D, n), whole(n, D), whole(n, D), whole(D, n),
        ],
        out_shape=[
            shaped(BF16, groups, n, width), shaped(BF16, groups, n, width),
            shaped(BF16, groups, width, n), shaped(BF16, groups, heads, n, n),
            shaped(BF16, groups, n, width), shaped(BF16, D, n), shaped(F32, n, D),
            shaped(BF16, n, D), shaped(BF16, D, n),
        ],
        scratch_shapes=[
            pltpu.VMEM((n, D), BF16), pltpu.VMEM((n, width), BF16),
            pltpu.VMEM((width, n), BF16), pltpu.VMEM((width, n), BF16),
            pltpu.VMEM((n, D), F32),
        ],
        compiler_params=pltpu.CompilerParams(vmem_limit_bytes=VMEM_LIMIT),
        name="attention_forward",
    )(length, x, g0, rows, bqv)


def run_feed_forward(length, cot, a2, a2t, h1, g1, g2, rows):
    n = cot.shape[0]
    groups, _, width = g1.shape
    return pl.pallas_call(
        feed_forward_both,
        grid=(groups,),
        in_specs=[
            SMEM_WHOLE, whole(n, D), whole(n, D), whole(D, n), whole(n, D),
            group(D, width), group(D, width), whole(16, D),
        ],
        out_specs=[
            whole(n, D), group(D, width), group(D, width), whole(n, D), whole(n, D),
            whole(D, n), whole(16, D),
        ],
        out_shape=[
            shaped(BF16, n, D), shaped(BF16, groups, D, width), shaped(BF16, groups, D, width),
            shaped(F32, n, D), shaped(BF16, n, D), shaped(BF16, D, n), shaped(F32, 16, D),
        ],
        scratch_shapes=[
            pltpu.VMEM((n, D), BF16), pltpu.VMEM((D, n), BF16), pltpu.VMEM((n, D), F32),
            pltpu.VMEM((n, D), F32), pltpu.VMEM((n, width), BF16), pltpu.VMEM((n, width), BF16),
        ],
        compiler_params=pltpu.CompilerParams(vmem_limit_bytes=VMEM_LIMIT),
        name="feed_forward_both",
    )(length, cot, a2, a2t, h1, g1, g2, rows)


def run_attention_backward(x, g0, rows, dh1, gb, gbt, q, v, kt, p, o, a1t):
    n = x.shape[0]
    groups, _, _, width = g0.shape
    heads = width // HEAD_DIM
    return pl.pallas_call(
        attention_backward,
        grid=(groups,),
        in_specs=[
            whole(n, D), group(4, D, width), whole(16, D), whole(n, D), whole(n, D),
            whole(D, n), group(n, width), group(n, width), group(width, n),
            group(heads, n, n), group(n, width), whole(D, n),
        ],
        out_specs=[group(4, D, width), whole(n, D), whole(8, D), group(8, width)],
        out_shape=[
            shaped(BF16, groups, 4, D, width), shaped(BF16, n, D), shaped(F32, 8, D),
            shaped(F32, groups, 8, width),
        ],
        scratch_shapes=[
            pltpu.VMEM((n, width), BF16), pltpu.VMEM((16, n), F32), pltpu.VMEM((width, n), F32),
            pltpu.VMEM((n, width), BF16), pltpu.VMEM((n, width), BF16),
            pltpu.VMEM((n, width), BF16), pltpu.VMEM((n, D), F32),
        ],
        compiler_params=pltpu.CompilerParams(vmem_limit_bytes=VMEM_LIMIT),
        name="attention_backward",
    )(x, g0, rows, dh1, gb, gbt, q, v, kt, p, o, a1t)


Z_DEV, Y_DEV, X_DEV, C_DEV = 4, 2, 2, 2


class Place:
    def __init__(self):
        dp, self.t = lax.axis_index("dp"), lax.axis_index("tensor")
        self.dp = dp
        self.z, self.y = dp // 2, dp % 2
        self.x, self.c = self.t // 2, self.t % 2
        self.other_y = 1 - self.y
        self.zs = [
            self.z,
            self.z + 1 - 2 * (self.z % 2),
            self.z + 2 - 4 * (self.z // 2),
            3 - self.z,
        ]
        self.ts = [
            self.t,
            self.t + 1 - 2 * (self.t % 2),
            self.t + 2 - 4 * (self.t // 2),
            3 - self.t,
        ]
        self.to_z = [dict(dp=z * 2 + self.y) for z in self.zs]
        self.to_y = dict(dp=self.z * 2 + self.other_y)
        self.to_x = dict(tensor=self.ts[2])
        self.same_t = self.to_z[1:] + [dict(dp=z * 2 + self.other_y) for z in self.zs]
        self.same_dp = [dict(tensor=t) for t in self.ts[1:]]
        self.to_core = dict(tensor=self.ts[1])

    def group(self, k):
        return lax.select(
            k == 0, self.ts[0],
            lax.select(k == 1, self.ts[1], lax.select(k == 2, self.ts[2], self.ts[3])),
        )

    def greet(self, others=None):
        barrier = pltpu.get_barrier_semaphore()
        others = others or self.to_z[1:] + [self.to_y, self.to_x, self.to_core]
        for device in others:
            pl.semaphore_signal(
                barrier, inc=1, device_id=device, device_id_type=pl.DeviceIdType.MESH
            )
        pl.semaphore_wait(barrier, len(others))


class Links:
    def __init__(self, send_sem, recv_sem):
        self.send_sem, self.recv_sem = send_sem, recv_sem
        self.copies = []

    def add(self, device, src, dst):
        number = len(self.copies)
        copy = pltpu.make_async_remote_copy(
            src_ref=src,
            dst_ref=dst,
            send_sem=self.send_sem.at[number],
            recv_sem=self.recv_sem.at[number],
            device_id=device,
            device_id_type=pl.DeviceIdType.MESH,
        )
        self.copies.append(copy)
        return copy

    def sent(self, *apart):
        for copy in self.copies:
            if all(copy is not other for other in apart):
                copy.wait_send()


def flat(copies):
    for item in copies:
        if isinstance(item, list):
            yield from flat(item)
        else:
            yield item


def start(*copies):
    for copy in flat(copies):
        copy.start()


def recv(*copies):
    for copy in flat(copies):
        copy.wait_recv()


class Gather:
    def __init__(self, links, place, own, full, order, single=True, last=True):
        every = slice(None)
        y, other = place.y, place.other_y

        def same(device, k, yy, to):
            return links.add(device, full(k, every, yy), full(to, every, yy))

        def along_z(k, yy, block):
            here, passed = full(k, place.z, yy), full(k, place.zs[2], yy)
            return [
                links.add(place.to_z[1], block, here),
                links.add(place.to_z[2], block, here),
                links.add(place.to_z[1], passed, passed),
            ]

        self.z = along_z(0, y, own)
        if order == X_Z_Y:
            self.first = [links.add(place.to_x, own, full(2, place.z, y))]
            self.far = along_z(2, y, full(2, place.z, y))
            blocks = [(0, y), (2, y), (0, other), (2, other)]
        else:
            blocks = [(0, y), (0, other), (2, y), (2, other)]
        if order == Y_Z_X:
            self.first = [links.add(place.to_y, own, full(0, place.z, y))]
            self.far = along_z(0, other, full(0, place.z, other))
        if order == Z_Y_X and single:
            self.first = [same(place.to_y, 0, y, 0)]
        if order == Z_Y_X and not single:
            self.first = [links.add(place.to_y, own, full(0, place.z, y))]
            for k in range(1, 4):
                block = full(0, place.zs[k], y)
                self.first.append(links.add(place.to_y, block, block))
        self.second = [
            same(place.to_y, k, yy, k) if order == X_Z_Y else same(place.to_x, k, yy, 2)
            for k, yy in blocks[: 2 if last else 1]
        ]
        if not last:
            blocks = [block for block in blocks if block[0] == 0]
        self.core = [same(place.to_core, k, yy, k + 1) for k, yy in blocks]


Z_Y_X, Y_Z_X, X_Z_Y = range(3)


def fused_forward(
    tie_ref, len_ref, tokens_ref, gains_ref, bias_ref, in_ref, out_ref, expand_ref,
    project_ref,
    gq_ref, gw_ref, flat1_ref, flat2_ref, rows_ref,
    q_ref, v_ref, kt_ref, p_ref, scale_ref, o_ref, a1t_out, h1_out, a2_out, a2t_out,
    own0_ref, ownw_ref, own1_ref, own2_ref, square_ref, vec_ref,
    all0_ref, allw_ref, w1_ref, w2_ref, vecs_ref, bqv_ref, x_ref, a1_ref, k_ref, qa_ref, vt_ref, ot_ref, a1t_ref, h1_ref, a2_ref, a2t_ref,
    send_sem, recv_sem, local_sem, flush_sem, row_sem,
):
    t = pl.program_id(0)
    n, _ = x_ref.shape
    width = allw_ref.shape[-1]
    heads = width // HEAD_DIM
    step = 256
    place = Place()
    length = len_ref[place.t]
    links = Links(send_sem, recv_sem)
    z, y, x, c = place.z, place.y, place.x, place.c
    mine_there = vecs_ref.at[z, y, x, c]
    column = vecs_ref.at[:, :, x, c]
    vec_one = [links.add(device, vec_ref, mine_there) for device in place.same_t]
    vec_two = [links.add(device, column, column) for device in place.same_dp]
    seg0 = Gather(
        links, place, own0_ref, lambda k, z, y: all0_ref.at[k, z, y], Z_Y_X, single=False
    )
    segw = Gather(links, place, ownw_ref, lambda k, z, y: allw_ref.at[k, z, y], Z_Y_X)
    seg1 = Gather(
        links, place, own1_ref, lambda k, z, y: w1_ref.at[k, z, y], Y_Z_X, last=False
    )
    seg2 = Gather(
        links, place, own2_ref, lambda k, z, y: w2_ref.at[k, z, y], X_Z_Y, last=False
    )
    flush = [
        [
            pltpu.make_async_copy(ref.at[k], flat.at[k], flush_sem.at[i, k])
            for k in range(3)
        ]
        for i, (ref, flat) in enumerate([(w1_ref, flat1_ref), (w2_ref, flat2_ref)])
    ]
    put_a1t = pltpu.make_async_copy(a1t_ref, a1t_out, local_sem.at[0])
    put_a2t = pltpu.make_async_copy(a2t_ref, a2t_out, local_sem.at[1])
    puts = []
    for i in range(n // step):
        rows = pl.ds(i * step, step)
        puts.append([
            pltpu.make_async_copy(h1_ref.at[rows], h1_out.at[rows], row_sem.at[0, i]),
            pltpu.make_async_copy(a2_ref.at[rows], a2_out.at[rows], row_sem.at[1, i]),
        ])
    fetch = pltpu.make_async_copy(tokens_ref.at[place.t], x_ref, local_sem.at[2])

    def relay_z(copies):
        recv(copies[1])
        start(copies[2])

    def pass_own(seg):
        recv(seg.z[0], seg.z[2])
        if seg is segw:
            start(seg.first)
        start(seg.second[0], seg.core[0])

    def pass_second(seg):
        recv(seg.second)
        if seg is seg2:
            start(seg.core[1])

    def pass_first(seg):
        recv(seg.first)
        if seg is segw:
            start(seg.second[1], seg.core[1])
        else:
            start(seg.far[1], seg.far[0])

    def pass_far(seg):
        recv(seg.far[0], seg.far[2])
        start(seg.core[1:] if seg is seg1 else [])

    def pass_core(seg, i):
        recv(seg.second[i])
        start(seg.core[2 + i])

    plan = [
        (0, 0, lambda: (pass_own(segw), pass_first(seg1), relay_z(seg2.z), pass_first(seg2))),
        (0, 3, lambda: (pass_first(segw), relay_z(seg1.z), pass_core(seg0, 0))),
        (1, 0, lambda: recv(seg0.core[:2])),
        (1, 1, lambda: relay_z(seg1.far)),
        (1, 3, lambda: pass_core(seg0, 1)),
        (1, 4, lambda: (recv(segw.core[:2]), pass_core(segw, 0), pass_own(seg2))),
        (2, 1, lambda: relay_z(seg2.far)),
        (2, 2, lambda: pass_core(segw, 1)),
        (2, 3, lambda: pass_own(seg1)),
        (3, 0, lambda: (recv(seg0.core[2:]), pass_far(seg1), flush[0][0].start())),
        (3, 2, lambda: (pass_second(seg2), flush[1][0].start())),
        (3, 3, lambda: (pass_far(seg2), flush[1][2].start())),
        (3, 4, lambda: recv(segw.core[2:])),
    ]

    def serve(point):
        for step, where, act in plan:
            if where == point:
                pl.when(t == step)(lambda act=act: (act(), None)[1])

    @pl.when(t == 0)
    def _():
        s0, s1, s2, s3 = tie_ref[0], tie_ref[1], tie_ref[2], tie_ref[3]
        fetch.start()
        square_ref[...] = jnp.zeros_like(square_ref)
        gain = gains_ref.shape[-1]
        square_ref[0:1, :gain] = gains_ref[s0].astype(F32)[0:1]
        square_ref[1:2, :gain] = gains_ref[s2].astype(F32)[1:2]
        kinds = [s0, s0, s0, s1, s2, s3, s2, s2, s2, s2]
        for i, source in enumerate(kinds):
            wide = bias_ref[i].astype(F32)
            here = lax.broadcasted_iota(jnp.int32, wide.shape, 0) == source
            square_ref[2 + i : 3 + i, :gain] = jnp.sum(
                jnp.where(here, wide, 0.0), 0, keepdims=True
            )
        vec_ref[...] = square_ref[...].T[:gain]
        for j in range(3):
            own0_ref[:, j * width : (j + 1) * width] = in_ref[s0, j]
        place.greet(place.same_t + place.same_dp)
        start(vec_one, seg0.z[1], seg0.z[0], seg0.first[0])
        vecs_ref[z, y, x, c] = vec_ref[...]
        ones = lax.broadcasted_iota(jnp.int32, (vt_ref.shape[1] - HEAD_DIM, n), 0) == 0
        for h in range(heads):
            vt_ref[h, HEAD_DIM:, :] = ones.astype(BF16)
        all0_ref[0, z, y] = own0_ref[...]
        ownw_ref[...] = out_ref[s1].T
        allw_ref[0, z, y] = ownw_ref[...]
        own1_ref[...] = expand_ref[s2]
        own2_ref[...] = project_ref[s3]
        w1_ref[0, z, y] = own1_ref[...]
        w2_ref[0, z, y] = own2_ref[...]
        recv(vec_one)
        start(vec_two)
        relay_z(seg0.z)
        start(seg0.first[2])
        recv(seg0.z[0])
        start(seg0.first[1], segw.z[1], segw.z[0], seg2.z[1])
        recv(vec_two)
        start(seg2.first)
        vecs = vecs_ref[...].reshape(D, vecs_ref.shape[-1]).T[:16]
        rows_ref[...] = vecs
        recv(seg0.z[2])
        start(seg0.first[3], seg1.first, seg0.second[0], seg0.core[0])
        for k in range(4):
            part = slice(k * width, (k + 1) * width)
            bqv_ref[k, 0:1, :width] = vecs[3:4, part]
            bqv_ref[k, 0:1, width : 2 * width] = jnp.zeros((1, width), F32)
            bqv_ref[k, 0:1, 2 * width :] = vecs[4:5, part]
        fetch.wait()

        @pl.loop(0, n // step)
        def _(b):
            rows = pl.ds(pl.multiple_of(b * step, step), step)
            wide = x_ref[rows, :].astype(F32)
            xhat, _ = norm_parts(wide)
            a1 = (xhat * rows_ref[0:1, :] + rows_ref[2:3, :]).astype(BF16)
            a1_ref[rows, :] = a1
            a1t_ref[:, rows] = a1.T
            h1_ref[rows, :] = wide + rows_ref[5:6, :]

        put_a1t.start()
        relay_z(segw.z)
        start(seg2.z[0], seg1.z[1], seg1.z[0])
        recv(seg0.first)
        start(seg0.second[1], seg0.core[1])

    serve(0)
    gq = all0_ref[t].reshape(D, 3 * width)
    gq_ref[0] = gq
    mine = place.group(t)
    qkv = dot_nn(a1_ref[...], gq) + bqv_ref[mine, 0:1, :]
    q = qkv[:, :width].astype(BF16) * jnp.asarray(HEAD_DIM ** -0.5, BF16)
    k = qkv[:, width : 2 * width].astype(BF16)
    v = qkv[:, 2 * width :].astype(BF16)
    q_ref[0] = q
    kt_ref[0] = k.T
    v_ref[0] = v
    vt = v.T
    for h in range(heads):
        vt_ref[h, :HEAD_DIM, :] = vt[h * HEAD_DIM : (h + 1) * HEAD_DIM]
    spare = k_ref.shape[1] - width
    dead = lax.broadcasted_iota(jnp.int32, (n, spare), 0) >= length
    first_column = lax.broadcasted_iota(jnp.int32, (n, spare), 1) == 0
    k_ref[:, :width] = k
    k_ref[:, width:] = jnp.where(first_column & dead, MASKED, 0.0).astype(BF16)
    qa_ref[:, :width] = q
    qa_ref[:, width:] = jnp.where(first_column, 1.0, 0.0).astype(BF16)

    serve(1)
    def scores(h, b):
        first, last = b * step, (b + 1) * step
        q = qa_ref[first:last, :]
        lane = lax.broadcasted_iota(jnp.int32, (1, q.shape[1]), 1)
        keep = head_mask((1, q.shape[1]), h) | (lane >= width)
        return dot_nt(k_ref[:last, :], jnp.where(keep, q, jnp.zeros((), BF16)))

    def attend(h, b, s):
        first, last = b * step, (b + 1) * step
        key = lax.broadcasted_iota(jnp.int32, (step, step), 0)
        query = lax.broadcasted_iota(jnp.int32, (step, step), 1)
        near = jnp.where(key <= query, s[first:], MASKED)
        top = jnp.max(near, 0, keepdims=True)
        if b:
            far = s[:first]
            top = jnp.maximum(top, jnp.max(far, 0, keepdims=True))
        e_near = jnp.exp((near - top).astype(BF16))
        p_ref[0, h, first:last, first:last] = e_near
        o = dot_nn(vt_ref[h, :, first:last], e_near)
        if b:
            e_far = jnp.exp((far - top).astype(BF16))
            p_ref[0, h, :first, first:last] = e_far
            o += dot_nn(vt_ref[h, :, :first], e_far)
        scale = 1.0 / o[HEAD_DIM : HEAD_DIM + 1]
        scale_ref[0, h : h + 1, first:last] = scale
        ot_ref[h * HEAD_DIM : (h + 1) * HEAD_DIM, first:last] = (
            o[:HEAD_DIM] * scale
        ).astype(BF16)

    scale_ref[0, heads:, :] = jnp.zeros((scale_ref.shape[1] - heads, n), F32)
    for h in range(heads):
        s = scores(h, 0)
        for b in range(n // step):
            ahead = scores(h, b + 1) if b + 1 < n // step else None
            attend(h, b, s)
            s = ahead
        serve(2 + h)

    gw_ref[0] = allw_ref[t].reshape(gw_ref.shape[1:])
    o = ot_ref[...].T
    o_ref[0] = o
    h1_ref[...] += dot_nt(o, gw_ref[0])

    @pl.when(t == 3)
    def _():
        for i, rows in enumerate(blocks(n, step)):
            xhat, _ = norm_parts(h1_ref[rows, :])
            a2 = (xhat * rows_ref[1:2, :] + rows_ref[6:7, :]).astype(BF16)
            a2_ref[rows, :] = a2
            a2t_ref[:, rows] = a2.T
            for put in puts[i]:
                put.start()
        put_a2t.start()
        recv(seg2.core)
        flush[1][1].start()
        recv(seg1.core)
        flush[0][1].start()
        pass_second(seg1)
        flush[0][2].start()
        links.sent()
        for copies in flush + puts + [[put_a1t, put_a2t]]:
            for copy in copies:
                copy.wait()


N_GATHER = 10 + 13 + 10 + 10 + 10
VMEM_WHOLE = pl.BlockSpec(memory_space=pltpu.VMEM)
ANY_WHOLE = pl.BlockSpec(memory_space=pl.ANY)


def run_fused_forward(tie, lengths, tokens, gains, biases, w_in, w_out, w_expand, w_project):
    groups, n, _ = tokens.shape
    depth, width = w_in.shape[-2:]
    heads = width // HEAD_DIM
    hidden = w_expand.shape[-1]
    w_project = w_project.transpose(0, 2, 1)
    biases = biases.transpose(1, 0, 2)
    own = gains.shape[-1]
    return pl.pallas_call(
        fused_forward,
        grid=(groups,),
        in_specs=[SMEM_WHOLE, SMEM_WHOLE, ANY_WHOLE] + [VMEM_WHOLE] * 6,
        out_specs=[
            group(D, 3 * width), group(D, width), ANY_WHOLE, ANY_WHOLE, VMEM_WHOLE,
            group(n, width), group(n, width), group(width, n), group(heads, n, n),
            group(8, n), group(n, width), ANY_WHOLE, ANY_WHOLE, ANY_WHOLE, ANY_WHOLE,
        ],
        out_shape=[
            shaped(BF16, groups, D, 3 * width), shaped(BF16, groups, D, width),
            shaped(BF16, groups, Z_DEV, Y_DEV, depth, hidden),
            shaped(BF16, groups, Z_DEV, Y_DEV, depth, hidden),
            shaped(F32, 16, D),
            shaped(BF16, groups, n, width), shaped(BF16, groups, n, width),
            shaped(BF16, groups, width, n), shaped(BF16, groups, heads, n, n),
            shaped(F32, groups, 8, n), shaped(BF16, groups, n, width), shaped(BF16, D, n), shaped(F32, n, D),
            shaped(BF16, n, D), shaped(BF16, D, n),
        ],
        scratch_shapes=[
            pltpu.VMEM((depth, 3 * width), BF16), pltpu.VMEM((depth, width), BF16),
            pltpu.VMEM((depth, hidden), BF16), pltpu.VMEM((depth, hidden), BF16),
            pltpu.VMEM((128, 128), F32), pltpu.VMEM((own, 128), F32),
            pltpu.VMEM((groups, Z_DEV, Y_DEV, depth, 3 * width), BF16),
            pltpu.VMEM((groups, Z_DEV, Y_DEV, depth, width), BF16),
            pltpu.VMEM((groups, Z_DEV, Y_DEV, depth, hidden), BF16),
            pltpu.VMEM((groups, Z_DEV, Y_DEV, depth, hidden), BF16),
            pltpu.VMEM((Z_DEV, Y_DEV, X_DEV, C_DEV, own, 128), F32),
            pltpu.VMEM((groups, 8, 3 * width), F32),
            pltpu.VMEM((n, D), BF16), pltpu.VMEM((n, D), BF16), pltpu.VMEM((n, 256), BF16),
            pltpu.VMEM((n, 256), BF16), pltpu.VMEM((heads, HEAD_DIM + 16, n), BF16),
            pltpu.VMEM((width, n), BF16),
            pltpu.VMEM((D, n), BF16), pltpu.VMEM((n, D), F32), pltpu.VMEM((n, D), BF16),
            pltpu.VMEM((D, n), BF16),
            pltpu.SemaphoreType.DMA((N_GATHER,)), pltpu.SemaphoreType.DMA((N_GATHER,)),
            pltpu.SemaphoreType.DMA((3,)), pltpu.SemaphoreType.DMA((2, 4)),
            pltpu.SemaphoreType.DMA((2, n // 256)),
        ],
        compiler_params=pltpu.CompilerParams(
            vmem_limit_bytes=VMEM_LIMIT, collective_id=0, has_side_effects=True
        ),
        name="fused_forward",
    )(tie, lengths, tokens, gains, biases, w_in, w_out, w_expand, w_project)


class Result:
    def __init__(self, links, place, own_ref, passing_ref, out_ref, step, sem, count):
        self.x, self.core, self.far, self.keep, self.keep_far = [], [], [], [], []
        for i in range(count):
            rows = pl.ds(i * step, step)
            mine, theirs = out_ref.at[place.t, rows], out_ref.at[place.ts[2], rows]
            own, passing = own_ref.at[rows], passing_ref.at[rows]
            self.x.append(links.add(place.to_x, own, passing))
            self.core.append(links.add(place.to_core, own, mine))
            self.far.append(links.add(place.to_core, passing, theirs))
            self.keep.append(pltpu.make_async_copy(own, mine, sem.at[0, i]))
            self.keep_far.append(pltpu.make_async_copy(passing, theirs, sem.at[1, i]))

    def send(self, i):
        start(self.x[i], self.core[i], self.keep[i])

    def pass_on(self, i):
        recv(self.x[i])
        start(self.far[i], self.keep_far[i])

    def finish(self):
        recv(self.core, self.far)
        for copy in self.keep + self.keep_far:
            copy.wait()


def low(value):
    return jnp.asarray(value, BF16)


def pair_order(i):
    return i + 1 - 2 * (i % 2)


def fused_feed_forward(
    len_ref, cot_ref, a2_ref, a2t_in, h1_in, far1_ref, far2_ref, rows_ref,
    result_out, rest_out, fold_ref, work_out, dh1_out, gb_out, gbt_out, sums_ref,
    gf_ref, gft_ref, feed_ref, da2_ref, h_ref, slope_ref, weights_ref, missing_ref, third_ref,
    stage_ref, land_ref, near_ref, cross_ref, a2t_ref, h1_ref, out_ref, work_ref,
    passing_ref, send_sem, recv_sem, local_sem, row_sem, result_sem,
):
    t = pl.program_id(0)
    n = gf_ref.shape[0]
    step = 256
    depth = stage_ref.shape[-2]
    place = Place()
    length = len_ref[place.t]
    links = Links(send_sem, recv_sem)
    y, other = place.y, place.other_y
    last = [
        links.add(place.to_x, far1_ref.at[0, :, other], missing_ref.at[0, 0]),
        links.add(place.to_y, far2_ref.at[2, :, y], missing_ref.at[1, 0]),
    ]
    last_core = [
        links.add(place.to_core, missing_ref.at[i, 0], missing_ref.at[i, 1]) for i in range(2)
    ]
    third = [
        links.add(place.to_core, far_ref.at[2, :, y], third_ref.at[i])
        for i, far_ref in enumerate([far1_ref, far2_ref])
    ]
    core = [
        [links.add(place.to_core, stage_ref.at[i], land_ref.at[s, i]) for i in range(2)]
        for s in range(2)
    ]
    cross = [
        links.add(place.to_y, near_ref.at[i, :, other], cross_ref.at[i]) for i in range(2)
    ]
    half = n // 2
    out = Result(links, place, out_ref, passing_ref, result_out, step, result_sem, half // step)
    fetch = pltpu.make_async_copy(cot_ref.at[place.t], gf_ref, local_sem.at[0])
    gb_ref, gbt_ref, dh1_ref = gf_ref, gft_ref, da2_ref
    late = [
        pltpu.make_async_copy(a2t_in, a2t_ref, local_sem.at[5]),
        pltpu.make_async_copy(h1_in, h1_ref, local_sem.at[6]),
    ]
    puts = []
    for i in range(n // step):
        rows = pl.ds(i * step, step)
        puts.append([
            pltpu.make_async_copy(ref.at[rows], out.at[rows], row_sem.at[j, i])
            for j, (ref, out) in enumerate(
                [(dh1_ref, dh1_out), (gb_ref, gb_out)]
            )
        ])
    put_gbt = pltpu.make_async_copy(gbt_ref, gbt_out, local_sem.at[7])
    put_work = pltpu.make_async_copy(work_ref, work_out, local_sem.at[8])
    put_rest = pltpu.make_async_copy(out_ref.at[pl.ds(half, half)], rest_out, local_sem.at[9])
    k = pair_order(t)
    mine = place.group(k)

    def load(group, whole, slot):
        for i, far_ref in enumerate([far1_ref, far2_ref]):
            there, here = far_ref.at[group], weights_ref.at[slot, i]
            if not whole:
                there, here = there.at[:, y], here.at[:, y]
            yield pltpu.make_async_copy(there, here, local_sem.at[1 + 2 * slot + i])

    def live_rows(b):
        at = b * step + lax.broadcasted_iota(jnp.int32, (step, 1), 0)
        return (at < length).astype(F32)

    @pl.when(t == 0)
    def _():
        fetch.start()
        for copy in load(1, True, 0):
            copy.start()
        for copy in late:
            copy.start()
        place.greet()
        start(last, third)
        sums_ref[...] = jnp.zeros_like(sums_ref)
        feed_ref[...] = jnp.zeros_like(feed_ref)
        da2_ref[...] = jnp.zeros_like(da2_ref)
        fetch.wait()

        @pl.loop(0, n // step)
        def _(b):
            rows = pl.ds(pl.multiple_of(b * step, step), step)
            g = (gf_ref[rows, :].astype(F32) * live_rows(b)).astype(BF16)
            gf_ref[rows, :] = g
            gft_ref[:, rows] = g.T
            sums_ref[7:8, :] += jnp.sum(g.astype(F32), 0, keepdims=True)

    def weights(slot):
        return [weights_ref[slot, i].reshape(D, -1) for i in range(2)]

    def bend(f):
        f = f.astype(BF16)
        f2 = f * f
        th = jnp.tanh(f * (low(SQRT_2_PI) + low(SQRT_2_PI * 0.044715) * f2))
        half = low(0.5) + low(0.5) * th
        slope = half + f * (low(0.5) - low(0.5) * th * th) * (
            low(SQRT_2_PI) + low(3 * SQRT_2_PI * 0.044715) * f2
        )
        return f * half, slope

    def forward(slot, mine):
        w1, w2 = weights(slot)
        bias = rows_ref[pl.ds(8 + mine, 1), :]
        for rows in blocks(n, step):
            h, slope = bend(dot_nn(a2_ref[rows, :], w1) + bias)
            h_ref[slot, rows, :] = h
            slope_ref[slot, rows, :] = slope
            feed_ref[rows, :] += dot_nt(h, w2)

    def backward(slot, mine):
        w1, w2 = weights(slot)
        column = jnp.zeros((1, w1.shape[1]), F32)
        for rows in blocks(n, step):
            dh = dot_nn(gf_ref[rows, :], w2)
            df = (dh * slope_ref[slot, rows, :].astype(F32)).astype(BF16)
            slope_ref[slot, rows, :] = df
            column += jnp.sum(df.astype(F32), 0, keepdims=True)
            da2_ref[rows, :] += dot_nt(df, w1)
        sums_ref[pl.ds(8 + mine, 1), :] = column

    def both_ways(slot, mine):
        w1, w2 = weights(slot)
        bias = rows_ref[pl.ds(8 + mine, 1), :]
        column = jnp.zeros((1, w1.shape[1]), F32)
        for rows in blocks(n, step):
            f = dot_nn(a2_ref[rows, :], w1) + bias
            dh = dot_nn(gf_ref[rows, :], w2)
            h, slope = bend(f)
            df = (dh * slope.astype(F32)).astype(BF16)
            h_ref[slot, rows, :] = h
            slope_ref[slot, rows, :] = df
            column += jnp.sum(df.astype(F32), 0, keepdims=True)
            feed_ref[rows, :] += dot_nt(h, w2)
            da2_ref[rows, :] += dot_nt(df, w1)
        sums_ref[pl.ds(8 + mine, 1), :] = column

    for i in range(2):
        @pl.when(t == i)
        def _():
            for copy in load(1 - i, True, i):
                copy.wait()
            if i == 0:
                for copy in load(0, True, 1):
                    copy.start()

    @pl.when(t < 2)
    def _():
        both_ways(t, mine)

    @pl.when(t == 2)
    def _():
        for copy in load(2, False, 1):
            copy.start()
        recv(last_core, third)
        for j in range(2):
            weights_ref[0, j, :, y] = third_ref[j]
            weights_ref[0, j, :, other] = missing_ref[j, 1]
        forward(0, place.ts[3])
        for copy in load(2, False, 1):
            copy.wait()
        for j in range(2):
            weights_ref[1, j, :, other] = missing_ref[j, 0]
        forward(1, place.ts[2])
        late[1].wait()
        for i, rows in enumerate(blocks(n, step)):
            total = h1_ref[rows, :] + (feed_ref[rows, :] + rows_ref[7:8, :])
            out_ref[rows, :] = (live_rows(i) * total).astype(BF16)
        put_rest.start()
        for i in range(half // step):
            out.send(i)
        backward(0, place.ts[3])

    @pl.when(t == 3)
    def _():
        backward(1, place.ts[2])
        out.pass_on(0)

    @pl.when(t == 1)
    def _():
        recv(last)
        start(last_core)

    @pl.when(t == 0)
    def _():
        late[0].wait()

    def weight_grad(left_ref, right_ref):
        value = dot_nn(left_ref[...], right_ref[...])
        return value.reshape(Z_DEV, Y_DEV, depth, value.shape[-1]).astype(BF16)

    grad1 = weight_grad(a2t_ref, slope_ref.at[t % 2])
    grad2 = weight_grad(gft_ref, h_ref.at[t % 2])

    def put(ref):
        ref[0] = grad1
        ref[1] = grad2

    def reduced(ref):
        return lambda i, s, z: (
            ref[i, z].astype(F32) + land_ref[s, i, z].astype(F32)
        ).astype(BF16)

    @pl.when(t == 0)
    def _():
        put(stage_ref)
        start(core[0])

    @pl.when(t == 1)
    def _():
        put(near_ref)
        recv(core[0])

        @pl.loop(0, Z_DEV)
        def _(z):
            for i in range(2):
                near_ref[i, z] = reduced(near_ref)(i, 0, z)

        start(cross)

    @pl.when(t == 2)
    def _():
        for copy in core[0]:
            copy.wait_send()
        put(stage_ref)
        start(core[1])

    @pl.when(t == 3)
    def _():
        put(work_ref)
        for i, rows in enumerate(blocks(n, step)):
            xhat, r = norm_parts(h1_ref[rows, :])
            da2 = da2_ref[rows, :]
            sums_ref[1:2, :] += jnp.sum(da2 * xhat, 0, keepdims=True)
            sums_ref[6:7, :] += jnp.sum(da2, 0, keepdims=True)
            dg = da2 * rows_ref[1:2, :]
            dv = r * (
                dg
                - jnp.mean(dg, -1, keepdims=True)
                - xhat * jnp.mean(dg * xhat, -1, keepdims=True)
            )
            dh1 = gf_ref[rows, :].astype(F32) + dv
            dh1_ref[rows, :] = dh1
            gb = dh1.astype(BF16)
            gb_ref[rows, :] = gb
            gbt_ref[:, rows] = gb.T
            sums_ref[5:6, :] += jnp.sum(gb.astype(F32), 0, keepdims=True)
            for copy in puts[i]:
                copy.start()
        put_gbt.start()
        recv(core[1])

        @pl.loop(0, Z_DEV)
        def _(z):
            for i in range(2):
                work_ref[i, z] = reduced(work_ref)(i, 1, z)

        put_work.start()
        recv(cross)

        @pl.loop(0, Z_DEV)
        def _(z):
            for i in range(2):
                fold_ref[i, z] = (
                    near_ref[i, z, y].astype(F32) + cross_ref[i, z].astype(F32)
                ).astype(BF16)

        out.pass_on(1)
        out.finish()
        links.sent(*core[0])
        for copies in puts + [[put_gbt, put_work, put_rest]]:
            for copy in copies:
                copy.wait()


def run_fused_feed_forward(lengths, cot, a2, a2t, h1, g1, g2, rows):
    n = cot.shape[1]
    groups, _, _, depth, hidden = g1.shape
    both = (2, Z_DEV, Y_DEV, depth, hidden)
    fold = (2, Z_DEV, depth, hidden)
    return pl.pallas_call(
        fused_feed_forward,
        grid=(groups,),
        in_specs=[SMEM_WHOLE, ANY_WHOLE, VMEM_WHOLE] + [ANY_WHOLE] * 4 + [VMEM_WHOLE],
        out_specs=[ANY_WHOLE] * 2 + [VMEM_WHOLE] + [ANY_WHOLE] * 4 + [VMEM_WHOLE],
        out_shape=[
            shaped(BF16, groups, n // 2, D), shaped(BF16, n // 2, D), shaped(BF16, *fold),
            shaped(BF16, *both), shaped(F32, n, D),
            shaped(BF16, n, D), shaped(BF16, D, n), shaped(F32, 16, D),
        ],
        scratch_shapes=[
            pltpu.VMEM((n, D), BF16), pltpu.VMEM((D, n), BF16), pltpu.VMEM((n, D), F32),
            pltpu.VMEM((n, D), F32), pltpu.VMEM((2, n, hidden), BF16),
            pltpu.VMEM((2, n, hidden), BF16),
            pltpu.VMEM((2,) + both, BF16),
            pltpu.VMEM((2,) + fold, BF16), pltpu.VMEM(fold, BF16), pltpu.VMEM(both, BF16),
            pltpu.VMEM((2,) + both, BF16),
            pltpu.VMEM(both, BF16), pltpu.VMEM(fold, BF16),
            pltpu.VMEM((D, n), BF16), pltpu.VMEM((n, D), F32), pltpu.VMEM((n, D), BF16),
            pltpu.VMEM(both, BF16), pltpu.VMEM((n // 2, D), BF16),
            pltpu.SemaphoreType.DMA((18,)), pltpu.SemaphoreType.DMA((18,)),
            pltpu.SemaphoreType.DMA((10,)), pltpu.SemaphoreType.DMA((2, n // 256)),
            pltpu.SemaphoreType.DMA((2, 2)),
        ],
        compiler_params=pltpu.CompilerParams(
            vmem_limit_bytes=VMEM_LIMIT, collective_id=1, has_side_effects=True
        ),
        name="fused_feed_forward",
    )(lengths, cot, a2, a2t, h1, g1, g2, rows)
class Reduce:
    def __init__(
        self, links, place, work, acc, cross_ref, far_ref, mid_ref, last_ref, side_ref,
        slots=(0, 1), split=False,
    ):
        self.place, self.work, self.acc = place, work, acc
        self.cross_ref, self.far_ref, self.mid_ref = cross_ref, far_ref, mid_ref
        self.last_ref, self.side_ref = last_ref, side_ref
        zs = place.zs
        self.y = {
            s: [
                links.add(place.to_y, work(s, zs[j], place.other_y), cross_ref.at[s, zs[j]])
                for j in (1, 3, 2, 0)
            ]
            for s in slots
        }
        self.z = [
            [
                links.add(place.to_z[1], acc(s, zs[1]), far_ref.at[s, 0]),
                links.add(place.to_z[1], acc(s, zs[3]), far_ref.at[s, 1]),
                links.add(place.to_z[2], mid_ref.at[s, 1], far_ref.at[s, 2]),
            ]
            for s in range(1 if split else 2)
        ]
        self.x = links.add(place.to_x, last_ref, side_ref)

    def fold_y(self, s, half):
        for i, j in [(0, 1), (1, 3), (2, 2), (3, 0)][2 * half : 2 * half + 2]:
            z = self.place.zs[j]
            recv(self.y[s][i])
            value = self.work(s, z, self.place.y)[...].astype(F32)
            self.acc(s, z)[...] = (value + self.cross_ref[s, z].astype(F32)).astype(BF16)
            if i < 2:
                start(self.z[s][i])

    def fold_z(self, s):
        recv(self.z[s][:2])
        for i in (1, 0):
            value = self.acc(s, self.place.zs[2 * i])[...].astype(F32)
            self.mid_ref[s, i] = (value + self.far_ref[s, i].astype(F32)).astype(BF16)
            if i:
                start(self.z[s][2])

    def own(self, s):
        recv(self.z[s][2])
        return self.mid_ref[s, 0].astype(F32) + self.far_ref[s, 2].astype(F32)

    def send_x(self):
        self.last_ref[...] = self.own(1).astype(BF16)
        start(self.x)

    def total(self):
        value = self.own(0)
        recv(self.x)
        return value + self.side_ref[...].astype(F32)


class ReduceHalves:
    def __init__(self, links, place, work, landings, last_ref):
        self.place, self.work = place, work
        self.cross, self.far, self.mid, self.far2, self.mid2, self.fin2, self.cross2 = landings
        self.last_ref = last_ref
        zs, half = place.zs, last_ref.shape[0] // 2
        self.low, self.high = pl.ds(0, half), pl.ds(half, half)
        every = slice(None)
        y, other = place.y, place.other_y
        self.y = [
            links.add(place.to_y, work.at[zs[j], other, self.low], self.cross.at[zs[j]])
            for j in (1, 3, 2, 0)
        ]
        self.z = [
            links.add(place.to_z[1], work.at[zs[1], y, self.low], self.far.at[0]),
            links.add(place.to_z[1], work.at[zs[3], y, self.low], self.far.at[1]),
            links.add(place.to_z[2], self.mid.at[1], self.far.at[2]),
        ]
        self.z2 = [
            links.add(place.to_z[1], work.at[zs[1], every, self.high], self.far2.at[0]),
            links.add(place.to_z[1], work.at[zs[3], every, self.high], self.far2.at[1]),
            links.add(place.to_z[2], self.mid2.at[1], self.far2.at[2]),
        ]
        self.y2 = links.add(place.to_y, self.fin2.at[other], self.cross2)

    def begin(self):
        start(self.y, self.z2[:2])

    def add(self, target, left, right):
        target[...] = (left[...].astype(F32) + right[...].astype(F32)).astype(BF16)

    def fold_y(self):
        y, zs = self.place.y, self.place.zs
        for i, j in enumerate((1, 3, 2, 0)):
            recv(self.y[i])
            block = self.work.at[zs[j], y, self.low]
            self.add(block, block, self.cross.at[zs[j]])
            if i < 2:
                start(self.z[i])

    def fold_high(self):
        recv(self.z2[:2])
        for i in (1, 0):
            block = self.work.at[self.place.zs[2 * i], :, self.high]
            self.add(self.mid2.at[i], block, self.far2.at[i])
            if i:
                start(self.z2[2])

    def cross_high(self):
        recv(self.z2[2])
        self.add(self.fin2, self.mid2.at[0], self.far2.at[2])
        start(self.y2)

    def fold_z(self):
        recv(self.z[:2])
        for i in (1, 0):
            block = self.work.at[self.place.zs[2 * i], self.place.y, self.low]
            self.add(self.mid.at[i], block, self.far.at[i])
            if i:
                start(self.z[2])

    def finish(self):
        recv(self.z[2])
        self.add(self.last_ref.at[self.low], self.mid.at[0], self.far.at[2])
        recv(self.y2)
        self.add(self.last_ref.at[self.high], self.fin2.at[self.place.y], self.cross2)


def fused_backward(
    tokens_ref, gq_in, gw_in, rows_ref, dh1_ref, gb_ref, gbt_in, q_in, v_in, kt_in,
    p_ref, scale_in, o_in, a1t_in, layer_in, fold_in, work_in, early_ref,
    out_ref, layerout_ref, part0_ref, partw_ref, part1_ref, part2_ref, total_ref,
    gq_ref, gw_ref, q_ref, v_ref, kt_ref, scale_ref, o_ref,
    a1t_ref, gbt_ref, layer_ref, fold_ref, work_ref, do_ref, delta_ref, dkv_ref, dqkv_ref, da1_ref, own_ref, passing_ref, passlayer_ref, bqv_ref,
    folded_ref, cross1_ref, far1_ref, mid1_ref, last1_ref, side1_ref,
    cross2_ref, far2_ref, mid2_ref, last2_ref, side2_ref,
    stagew_ref, landw_ref, workw_ref, crossw_ref, farw_ref, midw_ref, lastw_ref, sidew_ref,
    stage0_ref, land0_ref, work0_ref, cross0_ref, far0_ref, mid0_ref, last0_ref, side0_ref,
    sums_ref, sumland_ref,
    send_sem, recv_sem, local_sem, result_sem, group_sem, *tail_refs,
):
    t = pl.program_id(0)
    n = own_ref.shape[0]
    width = gw_ref.shape[-1]
    depth = part0_ref.shape[0]
    heads = width // HEAD_DIM
    step = n // 4
    place = Place()
    y = place.y
    links = Links(send_sem, recv_sem)
    k, i = group_and_block(t)
    mine = place.group(k)
    now = k % 2
    out = Result(links, place, own_ref, passing_ref, out_ref, step, result_sem.at[0], 4)
    layer = Result(links, place, layer_ref, passlayer_ref, layerout_ref, step, result_sem.at[1], 2)
    fetch = pltpu.make_async_copy(tokens_ref.at[place.t], own_ref, local_sem.at[0])
    fetch_layer, fetch_work, fetch_fold, fetch_gbt, fetch_a1t = [
        pltpu.make_async_copy(there, here, local_sem.at[1 + j])
        for j, (there, here) in enumerate([
            (layer_in, layer_ref), (work_in, work_ref), (fold_in, fold_ref),
            (gbt_in, gbt_ref), (a1t_in, a1t_ref),
        ])
    ]
    def operands(group):
        slot = group % 2
        pairs = [
            (gw_in, gw_ref), (scale_in, scale_ref), (o_in, o_ref), (v_in, v_ref),
            (q_in, q_ref), (kt_in, kt_ref), (gq_in, gq_ref),
        ]
        return [
            pltpu.make_async_copy(there.at[group], here.at[slot], group_sem.at[slot, j])
            for j, (there, here) in enumerate(pairs)
        ]

    corew = [links.add(place.to_core, stagew_ref, landw_ref.at[i]) for i in range(2)]
    core0 = [links.add(place.to_core, stage0_ref, land0_ref.at[i]) for i in range(2)]
    def half_done(i, *landing):
        return Reduce(
            links, place, lambda s, z, y: work_ref.at[i, z, y],
            lambda s, z: folded_ref.at[i, z] if s else fold_ref.at[i, z],
            *landing, slots=(1,),
        )

    seg1 = half_done(0, cross1_ref, far1_ref, mid1_ref, last1_ref, side1_ref)
    seg2 = half_done(1, cross2_ref, far2_ref, mid2_ref, last2_ref, side2_ref)
    segw = Reduce(
        links, place, lambda s, z, y: workw_ref.at[s, z, y],
        lambda s, z: workw_ref.at[s, z, y],
        crossw_ref, farw_ref, midw_ref, lastw_ref, sidew_ref,
    )
    seg0 = Reduce(
        links, place, lambda s, z, y: work0_ref.at[s, z, y],
        lambda s, z: work0_ref.at[s, z, y],
        cross0_ref, far0_ref, mid0_ref, last0_ref, side0_ref, slots=(0,), split=True,
    )
    tail = ReduceHalves(links, place, work0_ref.at[1], tail_refs, last0_ref)
    sum_core, sum_y, *sum_z, sum_x = [
        links.add(to, sums_ref.at[i], sumland_ref.at[j])
        for j, (i, to) in enumerate(
            zip([0, 1, 2, 2, 2, 3], [place.to_core, place.to_y] + place.to_z[1:] + [place.to_x])
        )
    ]

    early_copies = [
        corew[1], core0[1], *segw.y[0], *segw.y[1], *segw.z[0], *seg0.y[0], *seg0.z[0],
        out.x[3], out.core[3], *layer.x, *layer.core, *layer.far, seg1.x, seg2.x,
    ]
    for seg in (seg1, seg2):
        early_copies += [*seg.y[1], *seg.z[0], *seg.z[1]]

    def sent(copies):
        for copy in copies:
            copy.wait_send()

    def when(point):
        return pl.when(t == point)

    @when(0)
    def _():
        start(fetch_layer, operands(1), fetch_work, fetch_fold, fetch_gbt, operands(0))
        start(fetch, fetch_a1t)
        place.greet()
        fetch_layer.wait()
        for i in range(2):
            layer.send(i)
        fetch_work.wait()
        start(seg1.y[1], seg2.y[1])
        fetch_fold.wait()
        start(seg1.z[0][:2], seg2.z[0][:2])
        bqv_ref[...] = jnp.zeros_like(bqv_ref)
        sums_ref[0] = early_ref[...]
        da1_ref[...] = jnp.zeros_like(da1_ref)
        fetch_gbt.wait()

    def add_core():
        recv(corew[1])

        @pl.loop(0, Z_DEV)
        def _(z):
            workw_ref[1, z] = (
                workw_ref[1, z].astype(F32) + landw_ref[1, z].astype(F32)
            ).astype(BF16)

        start(segw.y[1])

    def wait(copies):
        for copy in copies:
            copy.wait()

    @when(0)
    def _():
        wait(operands(1))

    @when(4)
    def _():
        start(operands(3))
        wait(operands(0))

    @when(8)
    def _():
        start(operands(2))
        wait(operands(3))

    @when(9)
    def _():
        wait(operands(2))

    plan = [
        (2, 1, lambda: (seg1.fold_y(1, 0), seg1.fold_z(0))),
        (3, 1, lambda: layer.pass_on(0)),
        (4, 0, lambda: (seg1.fold_y(1, 1), seg2.fold_z(0))),
        (4, 1, lambda: layer.pass_on(1)),
        (5, 1, lambda: (seg1.fold_z(1), seg2.fold_y(1, 0))),
        (8, 0, lambda: seg2.fold_y(1, 1)),
        (8, 1, lambda: (seg1.send_x(), segw.fold_y(0, 0), segw.fold_y(0, 1))),
        (9, 0, add_core),
        (9, 1, lambda: (seg2.fold_z(1), seg0.fold_y(0, 0))),
        (10, 1, lambda: segw.fold_z(0)),
        (11, 1, lambda: (seg2.send_x(), seg0.fold_y(0, 1))),
        (12, 1, lambda: (segw.fold_y(1, 0), segw.fold_y(1, 1))),
        (13, 1, lambda: (seg0.fold_z(0), out.pass_on(3))),
        (14, 1, lambda: segw.fold_z(1)),
    ]

    def serve(point):
        for at, where, act in plan:
            if where == point:
                pl.when(t == at)(lambda act=act: (act(), None)[1])

    @pl.when((t == 0) | (t == 4) | (t == 8) | (t == 9))
    def _():
        pick = (
            lax.broadcasted_iota(jnp.int32, (8, width), 1) // HEAD_DIM
            == lax.broadcasted_iota(jnp.int32, (8, width), 0)
        ).astype(BF16)

        @pl.loop(0, n // step)
        def _(i):
            rows = pl.ds(pl.multiple_of(i * step, step), step)
            columns = scale_ref[now, :, rows].T
            lane = lax.broadcasted_iota(jnp.int32, (step, width), 1)
            scale = columns[:, heads - 1 : heads]
            for h in reversed(range(heads - 1)):
                scale = jnp.where(lane < (h + 1) * HEAD_DIM, columns[:, h : h + 1], scale)
            do = (dot_nn(gb_ref[rows, :], gw_ref[now]) * scale).astype(BF16)
            do_ref[now, rows, :] = do
            product = do.astype(F32) * o_ref[now, rows, :].astype(F32)
            high = product.astype(BF16)
            low = (product - high.astype(F32)).astype(BF16)
            delta_ref[now, :, rows] = dot_nt(pick, high) + dot_nt(pick, low)

        value = dot_nn(gbt_ref[...], o_ref[now]).reshape(Z_DEV, Y_DEV, depth, width)
        for s in range(2):
            @when(8 * s)
            def _():
                if s:
                    corew[0].wait_send()
                stagew_ref[...] = value.astype(BF16)
                start(corew[s])

        @when(4)
        def _():
            recv(corew[0])
            workw_ref[0] = (value + landw_ref[0].astype(F32)).astype(BF16)
            start(segw.y[0])

        @when(9)
        def _():
            workw_ref[1] = value.astype(BF16)

    serve(0)

    for ii in reversed(range(4)):
        @pl.when(i == ii)
        def _():
            first, last = ii * step, (ii + 1) * step
            do = do_ref[now, first:last, :]
            q = q_ref[now, first:last, :]
            v = v_ref[now, :last, :]
            lane = lax.broadcasted_iota(jnp.int32, (1, width), 1)
            dk, dv, dq = None, None, []
            for h in range(heads):
                low, high = h * HEAD_DIM, (h + 1) * HEAD_DIM
                here = (lane >= low) & (lane < high)
                p = p_ref[0, h, :last, :]
                dp = dot_nt(v, jnp.where(here, do, jnp.zeros((), BF16)))
                ds = p * (dp - delta_ref[now, h : h + 1, first:last]).astype(BF16)
                part = dot_nn(p, do)
                dv = part if dv is None else jnp.where(lane < low, dv, part)
                part = dot_nn(ds, q)
                dk = part if dk is None else jnp.where(lane < low, dk, part)
                dq.append(dot_nn(kt_ref[now, low:high, :last], ds))
            if ii == 3:
                dkv_ref[now, 0] = dk
                dkv_ref[now, 1] = dv
            else:
                dkv_ref[now, 0, :last, :] += dk
                dkv_ref[now, 1, :last, :] += dv
            dk = dkv_ref[now, 0, first:last, :].astype(BF16)
            dv = dkv_ref[now, 1, first:last, :].astype(BF16)
            dq = (jnp.concatenate(dq, 0) * HEAD_DIM ** -0.5).astype(BF16).T
            dqkv_ref[now, first:last, :width] = dq
            dqkv_ref[now, first:last, width : 2 * width] = dk
            dqkv_ref[now, first:last, 2 * width :] = dv
            bqv_ref[mine, 0:1, :] += jnp.sum(dq.astype(F32), 0, keepdims=True)
            bqv_ref[mine, 1:2, :] += jnp.sum(dv.astype(F32), 0, keepdims=True)
            da1_ref[first:last, :] += dot_nt(dqkv_ref[now, first:last, :], gq_ref[now])

    serve(1)

    @pl.when((t == 3) | (t == 7) | (t > 13))
    def _():
        @when(3)
        def _():
            fetch.wait()
            fetch_a1t.wait()

        value = dot_nn(a1t_ref[...], dqkv_ref[now]).reshape(Z_DEV, Y_DEV, depth, 3 * width)
        for s in range(2):
            @when(3 + 11 * s)
            def _():
                if s:
                    core0[0].wait_send()
                stage0_ref[...] = value.astype(BF16)
                start(core0[s])

            @when(7 + 8 * s)
            def _():
                recv(core0[s])
                work0_ref[s] = (value + land0_ref[s].astype(F32)).astype(BF16)
                if s:
                    tail.begin()
                else:
                    start(seg0.y[s])

    @pl.when((t > 8) & (t % 2 == 1))
    def _():
        rows = pl.ds(pl.multiple_of(i * step, step), step)
        xhat, r = norm_parts(own_ref[rows, :].astype(F32))
        da1 = da1_ref[rows, :]
        sums_ref[0, 0:1, :] += jnp.sum(da1 * xhat, 0, keepdims=True)
        sums_ref[0, 2:3, :] += jnp.sum(da1, 0, keepdims=True)
        dg = da1 * rows_ref[0:1, :]
        dv = r * (
            dg
            - jnp.mean(dg, -1, keepdims=True)
            - xhat * jnp.mean(dg * xhat, -1, keepdims=True)
        )
        own_ref[rows, :] = (dh1_ref[...] + dv).astype(BF16)
        for ii in range(4):
            @pl.when(i == ii)
            def _():
                out.send(ii)

    @when(15)
    def _():
        for s in range(4):
            sums_ref[0, 3:5, s * width : (s + 1) * width] = bqv_ref[s, 0:2, :]
        start(sum_core)
        segw.send_x()
        part1_ref[...] = seg1.total()
        part2_ref[...] = seg2.total()
        sent(early_copies)
        tail.fold_high()
        recv(sum_core)
        sums_ref[1] = sums_ref[0] + sumland_ref[0]
        start(sum_y)
        tail.fold_y()
        tail.cross_high()
        tail.fold_z()
        recv(sum_y)
        sums_ref[2] = sums_ref[1] + sumland_ref[1]
        start(sum_z)
        out.pass_on(2)
        tail.finish()
        start(seg0.x)
        recv(sum_z)
        sums_ref[3] = (sums_ref[2] + sumland_ref[2]) + (sumland_ref[3] + sumland_ref[4])
        start(sum_x)
        out.pass_on(1)
        partw_ref[...] = segw.total()
        layer.finish()
        out.pass_on(0)
        recv(sum_x)
        total_ref[...] = sums_ref[3] + sumland_ref[5]
        part0_ref[...] = seg0.total()
        out.finish()
        links.sent(corew[0], core0[0], *early_copies)


def group_and_block(t):
    early = t < 8
    return (
        jnp.where(early, 1 - t // 4, 3 - t % 2),
        3 - jnp.where(early, t % 4, jnp.maximum(t - 8, 0) // 2),
    )


def run_fused_backward(
    tokens, gq, gw, rows, dh1, gb, gbt, q, v, kt, p, scale, o, a1t, layer, fold, work, early
):
    groups, n, _ = tokens.shape
    width = gw.shape[-1]
    heads = width // HEAD_DIM
    hidden = fold.shape[-1]
    depth = D // (Z_DEV * Y_DEV)
    step = n // 4

    p_spec = pl.BlockSpec(
        (1, heads, n, step),
        lambda t: (group_and_block(t)[0], 0, 0, group_and_block(t)[1]),
    )

    copies = 12 + 6 + 4 + 15 + 2 * 11 + 8 + 11 + 6

    def landing(lanes):
        return [
            pltpu.VMEM((2, Z_DEV, depth, lanes), BF16),
            pltpu.VMEM((2, 3, depth, lanes), BF16), pltpu.VMEM((2, 2, depth, lanes), BF16),
            pltpu.VMEM((depth, lanes), BF16), pltpu.VMEM((depth, lanes), BF16),
        ]

    def working(lanes):
        block = (Z_DEV, Y_DEV, depth, lanes)
        return [pltpu.VMEM(block, BF16)] + [pltpu.VMEM((2,) + block, BF16)] * 2

    return pl.pallas_call(
        fused_backward,
        grid=(4 * groups,),
        in_specs=[
            ANY_WHOLE, ANY_WHOLE, ANY_WHOLE, VMEM_WHOLE,
            pl.BlockSpec((step, D), lambda t: (group_and_block(jnp.maximum(t, 8))[1], 0)),
            VMEM_WHOLE, ANY_WHOLE, ANY_WHOLE, ANY_WHOLE, ANY_WHOLE, p_spec,
            ANY_WHOLE, ANY_WHOLE, ANY_WHOLE, ANY_WHOLE, ANY_WHOLE, ANY_WHOLE, VMEM_WHOLE,
        ],
        out_specs=[ANY_WHOLE] * 2 + [VMEM_WHOLE] * 5,
        out_shape=[
            shaped(BF16, groups, n, D), shaped(BF16, groups, n // 2, D),
            shaped(F32, depth, 3 * width),
            shaped(F32, depth, width), shaped(F32, depth, hidden),
            shaped(F32, depth, hidden), shaped(F32, 16, D),
        ],
        scratch_shapes=[
            pltpu.VMEM((2, D, 3 * width), BF16), pltpu.VMEM((2, D, width), BF16),
            pltpu.VMEM((2, n, width), BF16), pltpu.VMEM((2, n, width), BF16),
            pltpu.VMEM((2, width, n), BF16), pltpu.VMEM((2, 8, n), F32),
            pltpu.VMEM((2, n, width), BF16),
            pltpu.VMEM((D, n), BF16), pltpu.VMEM((D, n), BF16), pltpu.VMEM((n // 2, D), BF16),
            pltpu.VMEM((2, Z_DEV, depth, hidden), BF16),
            pltpu.VMEM((2, Z_DEV, Y_DEV, depth, hidden), BF16),
            pltpu.VMEM((2, n, width), BF16),
            pltpu.VMEM((2, 8, n), F32), pltpu.VMEM((2, 2, n, width), F32),
            pltpu.VMEM((2, n, 3 * width), BF16), pltpu.VMEM((n, D), F32),
            pltpu.VMEM((n, D), BF16), pltpu.VMEM((n, D), BF16), pltpu.VMEM((n // 2, D), BF16),
            pltpu.VMEM((groups, 8, width), F32),
        ]
        + landing(hidden)[:1] + landing(hidden) + landing(hidden)
        + working(width) + landing(width)
        + working(3 * width) + landing(3 * width)
        + [
            pltpu.VMEM((4, 16, D), F32), pltpu.VMEM((6, 16, D), F32),
            pltpu.SemaphoreType.DMA((copies,)), pltpu.SemaphoreType.DMA((copies,)),
            pltpu.SemaphoreType.DMA((6,)), pltpu.SemaphoreType.DMA((2, 2, 4)),
            pltpu.SemaphoreType.DMA((2, 7)),
            pltpu.VMEM((Z_DEV, depth // 2, 3 * width), BF16),
            pltpu.VMEM((3, depth // 2, 3 * width), BF16),
            pltpu.VMEM((2, depth // 2, 3 * width), BF16),
            pltpu.VMEM((3, Y_DEV, depth // 2, 3 * width), BF16),
            pltpu.VMEM((2, Y_DEV, depth // 2, 3 * width), BF16),
            pltpu.VMEM((Y_DEV, depth // 2, 3 * width), BF16),
            pltpu.VMEM((depth // 2, 3 * width), BF16),
        ],
        compiler_params=pltpu.CompilerParams(
            vmem_limit_bytes=VMEM_LIMIT, collective_id=2, has_side_effects=True
        ),
        name="fused_backward",
    )(tokens, gq, gw, rows, dh1, gb, gbt, q, v, kt, p, scale, o, a1t, layer, fold, work, early)


def place_gradients(
    tie_ref, sums_ref, part0_ref, partw_ref, part1_ref, part2_ref, near_out_ref, near_rest_ref,
    near_grad_ref, far_out_ref, far_grad_ref, gains_ref, bias_ref, in_ref, out_ref, expand_ref,
    project_ref,
):
    half = near_out_ref.shape[1]
    far_out_ref[0, :half] = near_out_ref[0]
    far_out_ref[0, half:] = near_rest_ref[0]
    far_grad_ref[...] = near_grad_ref[...]
    own = gains_ref.shape[-1]
    width = partw_ref.shape[-1]

    @pl.when(pl.program_id(0) == 0)
    def _():
        first = (lax.axis_index("dp") * 4 + lax.axis_index("tensor")) * own
        feature = lax.broadcasted_iota(jnp.int32, (D, 128), 0)
        lane = lax.broadcasted_iota(jnp.int32, (D, 128), 1)
        chosen = ((feature == first + lane) & (lane < own)).astype(F32)
        sums = lax.dot_general(
            sums_ref[...], chosen, (((1,), (0,)), ((), ())),
            precision=lax.Precision.HIGHEST, preferred_element_type=F32,
        )[:, :own]
        s0, s1, s2, s3 = tie_ref[0], tie_ref[1], tie_ref[2], tie_ref[3]
        w_out = partw_ref[...].T

        def at(source, wanted, value):
            return jnp.where(source == wanted, value, jnp.zeros_like(value))

        row = lax.broadcasted_iota(jnp.int32, (NSRC, own), 0)
        for i, wanted in enumerate([s0, s0, s0, s1, s2, s3, s2, s2, s2, s2]):
            bias_ref[i] = jnp.where(row == wanted, sums[2 + i : 3 + i], 0.0)
        for s in range(NSRC):
            gains_ref[s, 0:1] = at(s, s0, sums[0:1])
            gains_ref[s, 1:2] = at(s, s2, sums[1:2])
            for j in range(3):
                in_ref[s, j] = at(s, s0, part0_ref[:, j * width : (j + 1) * width])
            out_ref[s] = at(s, s1, w_out)
            expand_ref[s] = at(s, s2, part1_ref[...])
            project_ref[s] = at(s, s3, part2_ref[...])


def run_place_gradients(tie, sums, part0, partw, part1, part2, out, rest, grad, like):
    slots, n, _ = grad.shape
    gains, biases, w_in, w_out, w_expand, w_project = [item.shape for item in like]
    shapes = [
        gains, (biases[1], biases[0], biases[2]), w_in, w_out, w_expand,
        (w_project[0], w_project[2], w_project[1]),
    ]
    out, grad, gains, biases, w_in, w_out, w_expand, w_project = pl.pallas_call(
        place_gradients,
        grid=(slots,),
        in_specs=[SMEM_WHOLE] + [VMEM_WHOLE] * 5
        + [group(n // 2, D), group(n // 2, D), group(n, D)],
        out_specs=[group(n, D), group(n, D)] + [VMEM_WHOLE] * 6,
        out_shape=[shaped(BF16, slots, n, D)] * 2 + [shaped(F32, *item) for item in shapes],
        compiler_params=pltpu.CompilerParams(vmem_limit_bytes=VMEM_LIMIT),
        name="place_gradients",
    )(tie, sums, part0, partw, part1, part2, out, rest, grad)
    biases = biases.transpose(1, 0, 2)
    return out, grad, gains, biases, w_in, w_out, w_expand, w_project.transpose(0, 2, 1)


def plain_step(
    tokens, lengths, tie_map, norm_gains, bias_rows, attention_in, attention_out,
    expand_weight, project_weight, cotangent,
):
    slot_rows = tokens.shape[0] // lengths.shape[0]
    me = lax.axis_index("tensor")
    in_local = lax.dynamic_index_in_dim(attention_in, tie_map[0], 0, keepdims=False)
    out_local = lax.dynamic_index_in_dim(attention_out, tie_map[1], 0, keepdims=False)
    expand_local = lax.dynamic_index_in_dim(expand_weight, tie_map[2], 0, keepdims=False)
    project_local = lax.dynamic_index_in_dim(project_weight, tie_map[3], 0, keepdims=False)
    local0 = jnp.concatenate([in_local, out_local.T[None]], 0)
    row_kinds = jnp.array([0, 0, 0, 1, 2, 3] + [2] * (FF // D), dtype=jnp.int32)
    gain_kinds = jnp.array([0, 2], dtype=jnp.int32)
    gain_pick = norm_gains[tie_map[gain_kinds], jnp.arange(2)]
    bias_pick = bias_rows[tie_map[row_kinds], jnp.arange(row_kinds.shape[0])]
    vectors = jnp.concatenate([gain_pick, bias_pick], 0)
    x = lax.dynamic_slice_in_dim(tokens, me * slot_rows, slot_rows, 0)
    cot = lax.dynamic_slice_in_dim(cotangent, me * slot_rows, slot_rows, 0)
    length = lax.dynamic_slice_in_dim(lengths, me, 1, 0)
    rows = lax.all_gather(vectors, ("dp", "tensor"), axis=1, tiled=True).astype(F32)
    rows = jnp.concatenate([rows, jnp.zeros((4, D), F32)], 0)

    def gathered(piece, axis):
        piece = lax.all_gather(piece, "dp", axis=axis, tiled=True)
        return lax.all_gather(piece, "tensor", axis=0)

    g0 = gathered(local0, 1)
    g1 = gathered(expand_local, 0)
    g2 = gathered(project_local.T, 0)
    groups, width = g0.shape[0], g0.shape[-1]
    bqv = rows[3:5].reshape(2, groups, width).transpose(1, 0, 2)
    q, v, kt, p, o, a1t, h1, a2, a2t = run_attention_forward(length, x, g0, rows, bqv)
    out, d1, d2, dh1, gb, gbt, sums = run_feed_forward(length, cot, a2, a2t, h1, g1, g2, rows)
    d0, xg, sums_in, sums_qv = run_attention_backward(
        x, g0, rows, dh1, gb, gbt, q, v, kt, p, o, a1t
    )
    layer_out = lax.all_gather(out, "tensor", axis=0, tiled=True)
    tokens_grad = lax.all_gather(xg, "tensor", axis=0, tiled=True)

    def scattered(piece, axis):
        piece = lax.psum_scatter(piece, "tensor", scatter_dimension=0)
        return lax.psum_scatter(piece, "dp", scatter_dimension=axis, tiled=True).astype(F32)

    part0 = scattered(d0, 1)
    part1 = scattered(d1, 0)
    part2 = scattered(d2, 0)
    qv = sums_qv[:, :2].transpose(1, 0, 2).reshape(2, D)
    sums = jnp.concatenate(
        [sums_in[0:1], sums[1:2], sums_in[1:2], qv, sums[5:12]], 0
    )
    sums = lax.psum_scatter(sums, ("dp", "tensor"), scatter_dimension=1, tiled=True)
    return layer_out, tokens_grad, *placed(tie_map, sums, part0, part1, part2)


def fused_step(
    tokens, lengths, tie_map, norm_gains, bias_rows, attention_in, attention_out,
    expand_weight, project_weight, cotangent,
):
    slots = lengths.shape[0]
    tokens = tokens.reshape(slots, -1, D)
    cotangent = cotangent.reshape(slots, -1, D)
    gq, gw, g1, g2, rows, q, v, kt, p, scale, o, a1t, h1, a2, a2t = run_fused_forward(
        tie_map, lengths, tokens, norm_gains, bias_rows, attention_in, attention_out,
        expand_weight, project_weight,
    )
    out, layer, fold, work, dh1, gb, gbt, early = run_fused_feed_forward(
        lengths, cotangent, a2, a2t, h1, g1, g2, rows
    )
    grad, rest, part0, partw, part1, part2, sums = run_fused_backward(
        tokens, gq, gw, rows, dh1, gb, gbt, q, v, kt, p, scale, o, a1t, layer, fold,
        work, early,
    )
    out, grad, *placed_grads = run_place_gradients(
        tie_map, sums, part0, partw, part1, part2, out, rest, grad,
        (norm_gains, bias_rows, attention_in, attention_out, expand_weight, project_weight),
    )
    return out.reshape(-1, D), grad.reshape(-1, D), *placed_grads


def placed(tie_map, sums, part0, part1, part2):
    source = jnp.arange(NSRC, dtype=jnp.int32)

    def place(piece, which):
        pick = (source == tie_map[which]).reshape((NSRC,) + (1,) * piece.ndim)
        return jnp.where(pick, piece[None], 0.0)

    def place_rows(piece, kinds):
        pick = source[:, None] == tie_map[jnp.array(kinds, dtype=jnp.int32)][None, :]
        return jnp.where(pick[:, :, None], piece[None], 0.0)

    return (
        place_rows(sums[:2], [0, 2]),
        place_rows(sums[2:], [0, 0, 0, 1, 2, 3] + [2] * (FF // D)),
        place(part0[:3], 0),
        place(part0[3].T, 1),
        place(part1, 2),
        place(part2.T, 3),
    )


def solution(mesh):
    fused = mesh.shape["dp"] == Z_DEV * Y_DEV and mesh.shape["tensor"] == X_DEV * C_DEV
    return jax.shard_map(
        fused_step if fused else plain_step,
        mesh=mesh,
        in_specs=(
            P("dp", None),
            P("dp"),
            P(),
            P(None, None, ("dp", "tensor")),
            P(None, None, ("dp", "tensor")),
            P(None, None, "dp", "tensor"),
            P(None, "tensor", "dp"),
            P(None, "dp", "tensor"),
            P(None, "tensor", "dp"),
            P("dp", None),
        ),
        out_specs=(
            P("dp", None),
            P("dp", None),
            P(None, None, ("dp", "tensor")),
            P(None, None, ("dp", "tensor")),
            P(None, None, "dp", "tensor"),
            P(None, "tensor", "dp"),
            P(None, "dp", "tensor"),
            P(None, "tensor", "dp"),
        ),
        check_vma=False,
    )
```

```python
import jax
import jax.numpy as jnp
from jax import lax
from jax.experimental import pallas as pl
from jax.experimental.pallas import tpu as pltpu
from jax.sharding import PartitionSpec as P

D = 768
HEAD_DIM = 64
FF = 3072
NSRC = 4
EPS = 1e-05
MASKED = -1e30
F32 = jnp.float32
BF16 = jnp.bfloat16
VMEM_LIMIT = 60 * 1024 * 1024


def dot_nn(a, b):
    return lax.dot_general(a, b, (((1,), (0,)), ((), ())), preferred_element_type=F32)


def dot_nt(a, b):
    return lax.dot_general(a, b, (((1,), (1,)), ((), ())), preferred_element_type=F32)


def norm_parts(v):
    center = jnp.mean(v, -1, keepdims=True)
    centered = v - center
    r = lax.rsqrt(jnp.mean(centered * centered, -1, keepdims=True) + EPS)
    return centered * r, r


def head_mask(shape, h):
    lane = lax.broadcasted_iota(jnp.int32, shape, 1)
    return (lane >= h * HEAD_DIM) & (lane < (h + 1) * HEAD_DIM)


def blocks(total, size):
    return [slice(i * size, (i + 1) * size) for i in range(total // size)]


def attention_forward(
    len_ref, x_ref, g_ref, rows_ref, bqv_ref,
    q_ref, v_ref, kt_ref, p_ref, o_ref, a1t_ref, h1_ref, a2_ref, a2t_ref,
    a1_ref, k_ref, vt_ref, ot_ref, attn_ref,
):
    t = pl.program_id(0)
    n = x_ref.shape[0]
    width = g_ref.shape[-1]
    heads = width // HEAD_DIM
    step = 256
    length = len_ref[0]

    @pl.when(t == 0)
    def _():
        @pl.loop(0, n // step)
        def _(b):
            rows = pl.ds(pl.multiple_of(b * step, step), step)
            xhat, _ = norm_parts(x_ref[rows, :].astype(F32))
            a1 = xhat * rows_ref[0:1, :] + rows_ref[2:3, :]
            a1_ref[rows, :] = a1.astype(BF16)
            a1t_ref[:, rows] = a1.astype(BF16).T
            attn_ref[rows, :] = x_ref[rows, :].astype(F32) + rows_ref[5:6, :]

    @pl.loop(0, n // step)
    def _(b):
        rows = pl.ds(pl.multiple_of(b * step, step), step)
        a1 = a1_ref[rows, :]
        q = (dot_nn(a1, g_ref[0, 0]) + bqv_ref[0, 0:1, :]).astype(BF16)
        q_ref[0, rows, :] = q * jnp.asarray(HEAD_DIM ** -0.5, BF16)
        k = dot_nn(a1, g_ref[0, 1]).astype(BF16)
        k_ref[rows, :] = k
        kt_ref[0, :, rows] = k.T
        v = (dot_nn(a1, g_ref[0, 2]) + bqv_ref[0, 1:2, :]).astype(BF16)
        v_ref[0, rows, :] = v
        vt_ref[:, rows] = v.T

    for h in range(heads):
        k = k_ref[...]
        k = jnp.where(head_mask(k.shape, h), k, jnp.zeros_like(k))
        for b in range(n // step):
            first, last = b * step, (b + 1) * step
            q = q_ref[0, first:last, :]
            key = lax.broadcasted_iota(jnp.int32, (last, step), 0)
            query = lax.broadcasted_iota(jnp.int32, (step, step), 1) + first
            s = dot_nt(k[:last], q)
            near = jnp.where(
                (key[first:] <= query) & (key[first:] < length), s[first:], MASKED
            )
            if b:
                far = jnp.where(key[:first] < length, s[:first], MASKED)
                top = jnp.maximum(
                    jnp.max(far, 0, keepdims=True), jnp.max(near, 0, keepdims=True)
                )
                e_far = jnp.exp(far - top)
                e_near = jnp.exp(near - top)
                total = jnp.sum(e_far, 0, keepdims=True) + jnp.sum(e_near, 0, keepdims=True)
                scale = 1.0 / total
                p_ref[0, h, :first, first:last] = (e_far * scale).astype(BF16)
            else:
                top = jnp.max(near, 0, keepdims=True)
                e_near = jnp.exp(near - top)
                scale = 1.0 / jnp.sum(e_near, 0, keepdims=True)
            p_ref[0, h, first:last, first:last] = (e_near * scale).astype(BF16)
            ot_ref[h * HEAD_DIM : (h + 1) * HEAD_DIM, first:last] = dot_nn(
                vt_ref[h * HEAD_DIM : (h + 1) * HEAD_DIM, :last],
                p_ref[0, h, :last, first:last],
            ).astype(BF16)

    @pl.loop(0, n // step)
    def _(b):
        rows = pl.ds(pl.multiple_of(b * step, step), step)
        o = ot_ref[:, rows].T
        o_ref[0, rows, :] = o
        attn_ref[rows, :] += dot_nt(o, g_ref[0, 3])

    @pl.when(t == pl.num_programs(0) - 1)
    def _():
        @pl.loop(0, n // step)
        def _(b):
            rows = pl.ds(pl.multiple_of(b * step, step), step)
            h1 = attn_ref[rows, :]
            h1_ref[rows, :] = h1
            xhat, _ = norm_parts(h1)
            a2 = (xhat * rows_ref[1:2, :] + rows_ref[6:7, :]).astype(BF16)
            a2_ref[rows, :] = a2
            a2t_ref[:, rows] = a2.T


SQRT_2_PI = 0.7978845608028654


def feed_forward_both(
    len_ref, c_ref, a2_ref, a2t_ref, h1_ref, w1_ref, w2_ref, rows_ref,
    out_ref, d1_ref, d2_ref, dh1_ref, gb_ref, gbt_ref, sums_ref,
    gf_ref, gft_ref, feed_ref, da2_ref, h_ref, df_ref,
):
    t = pl.program_id(0)
    n = c_ref.shape[0]
    step = 256
    length = len_ref[0]

    @pl.when(t == 0)
    def _():
        sums_ref[...] = jnp.zeros_like(sums_ref)

        @pl.loop(0, n // step)
        def _(b):
            rows = pl.ds(pl.multiple_of(b * step, step), step)
            place = b * step + lax.broadcasted_iota(jnp.int32, (step, 1), 0)
            live = (place < length).astype(F32)
            g = (c_ref[rows, :].astype(F32) * live).astype(BF16)
            gf_ref[rows, :] = g
            gft_ref[:, rows] = g.T
            sums_ref[7:8, :] += jnp.sum(g.astype(F32), 0, keepdims=True)

    bias = rows_ref[pl.ds(8 + t, 1), :]

    @pl.loop(0, n // step)
    def _(b):
        rows = pl.ds(pl.multiple_of(b * step, step), step)
        f = dot_nn(a2_ref[rows, :], w1_ref[0]) + bias
        dh = dot_nn(gf_ref[rows, :], w2_ref[0])
        f2 = f * f
        th = jnp.tanh(f * (SQRT_2_PI + (SQRT_2_PI * 0.044715) * f2))
        half = 0.5 + 0.5 * th
        h = (f * half).astype(BF16)
        slope = half + f * (0.5 - 0.5 * th * th) * (
            SQRT_2_PI + (3 * SQRT_2_PI * 0.044715) * f2
        )
        df = (dh * slope).astype(BF16)
        h_ref[rows, :] = h
        df_ref[rows, :] = df
        sums_ref[pl.ds(8 + t, 1), :] += jnp.sum(df.astype(F32), 0, keepdims=True)
        feed = dot_nt(h, w2_ref[0])
        da2 = dot_nt(df, w1_ref[0])

        @pl.when(t == 0)
        def _():
            feed_ref[rows, :] = feed
            da2_ref[rows, :] = da2

        @pl.when(t > 0)
        def _():
            feed_ref[rows, :] += feed
            da2_ref[rows, :] += da2

    @pl.loop(0, D // step)
    def _(b):
        rows = pl.ds(pl.multiple_of(b * step, step), step)
        d1_ref[0, rows, :] = dot_nn(a2t_ref[rows, :], df_ref[...]).astype(BF16)
        d2_ref[0, rows, :] = dot_nn(gft_ref[rows, :], h_ref[...]).astype(BF16)

    @pl.when(t == pl.num_programs(0) - 1)
    def _():
        @pl.loop(0, n // step)
        def _(b):
            rows = pl.ds(pl.multiple_of(b * step, step), step)
            place = b * step + lax.broadcasted_iota(jnp.int32, (step, 1), 0)
            live = (place < length).astype(F32)
            h1 = h1_ref[rows, :]
            out_ref[rows, :] = (live * (h1 + (feed_ref[rows, :] + rows_ref[7:8, :]))).astype(BF16)
            xhat, r = norm_parts(h1)
            da2 = da2_ref[rows, :]
            sums_ref[1:2, :] += jnp.sum(da2 * xhat, 0, keepdims=True)
            sums_ref[6:7, :] += jnp.sum(da2, 0, keepdims=True)
            dg = da2 * rows_ref[1:2, :]
            dv = r * (
                dg
                - jnp.mean(dg, -1, keepdims=True)
                - xhat * jnp.mean(dg * xhat, -1, keepdims=True)
            )
            dh1 = live * c_ref[rows, :].astype(F32) + dv
            dh1_ref[rows, :] = dh1
            gb = dh1.astype(BF16)
            gb_ref[rows, :] = gb
            gbt_ref[:, rows] = gb.T
            sums_ref[5:6, :] += jnp.sum(gb.astype(F32), 0, keepdims=True)


def attention_backward(
    x_ref, g_ref, rows_ref, dh1_ref, gb_ref, gbt_ref, q_ref, v_ref, kt_ref, p_ref,
    o_ref, a1t_ref,
    d0_ref, xg_ref, sums_ref, bqv_ref,
    do_ref, delta_ref, dqt_ref, dq_ref, dk_ref, dv_ref, da1_ref,
):
    t = pl.program_id(0)
    n = x_ref.shape[0]
    width = g_ref.shape[-1]
    heads = width // HEAD_DIM
    step = 256
    pick = (
        lax.broadcasted_iota(jnp.int32, (16, width), 1) // HEAD_DIM
        == lax.broadcasted_iota(jnp.int32, (16, width), 0)
    ).astype(BF16)

    @pl.loop(0, n // step)
    def _(b):
        rows = pl.ds(pl.multiple_of(b * step, step), step)
        do = dot_nn(gb_ref[rows, :], g_ref[0, 3]).astype(BF16)
        do_ref[rows, :] = do
        prod = do.astype(F32) * o_ref[0, rows, :].astype(F32)
        high = prod.astype(BF16)
        low = (prod - high.astype(F32)).astype(BF16)
        delta_ref[:, rows] = dot_nt(pick, high) + dot_nt(pick, low)

    dqt_ref[...] = jnp.zeros_like(dqt_ref)
    for b in range(n // step):
        first, last = b * step, (b + 1) * step
        do = do_ref[first:, :]
        q = q_ref[0, first:, :]
        v = v_ref[0, first:last, :]
        dk, dv = None, None
        for h in range(heads):
            mine = head_mask((1, width), h)
            zero = jnp.zeros((), BF16)
            p = p_ref[0, h, first:last, first:]
            dp = dot_nt(jnp.where(mine, v, zero), do)
            ds = (p.astype(F32) * (dp - delta_ref[h : h + 1, first:])).astype(BF16)
            part = dot_nn(p, jnp.where(mine, do, zero))
            dv = part if dv is None else dv + part
            part = dot_nn(ds, jnp.where(mine, q, zero))
            dk = part if dk is None else dk + part
            head = slice(h * HEAD_DIM, (h + 1) * HEAD_DIM)
            dqt_ref[head, first:] += dot_nn(kt_ref[0, head, first:last], ds)
        dk_ref[first:last, :] = dk.astype(BF16)
        dv_ref[first:last, :] = dv.astype(BF16)

    @pl.when(t == 0)
    def _():
        da1_ref[...] = jnp.zeros_like(da1_ref)

    bqv_ref[...] = jnp.zeros_like(bqv_ref)

    @pl.loop(0, n // step)
    def _(b):
        rows = pl.ds(pl.multiple_of(b * step, step), step)
        dq = (dqt_ref[:, rows] * HEAD_DIM ** -0.5).astype(BF16).T
        dk = dk_ref[rows, :]
        dv = dv_ref[rows, :]
        dq_ref[rows, :] = dq
        bqv_ref[0, 0:1, :] += jnp.sum(dq.astype(F32), 0, keepdims=True)
        bqv_ref[0, 1:2, :] += jnp.sum(dv.astype(F32), 0, keepdims=True)
        da1_ref[rows, :] += (
            dot_nt(dq, g_ref[0, 0]) + dot_nt(dk, g_ref[0, 1]) + dot_nt(dv, g_ref[0, 2])
        )

    @pl.loop(0, D // step)
    def _(b):
        rows = pl.ds(pl.multiple_of(b * step, step), step)
        a1t = a1t_ref[rows, :]
        d0_ref[0, 0, rows, :] = dot_nn(a1t, dq_ref[...]).astype(BF16)
        d0_ref[0, 1, rows, :] = dot_nn(a1t, dk_ref[...]).astype(BF16)
        d0_ref[0, 2, rows, :] = dot_nn(a1t, dv_ref[...]).astype(BF16)
        d0_ref[0, 3, rows, :] = dot_nn(gbt_ref[rows, :], o_ref[0]).astype(BF16)

    @pl.when(t == pl.num_programs(0) - 1)
    def _():
        sums_ref[...] = jnp.zeros_like(sums_ref)

        @pl.loop(0, n // step)
        def _(b):
            rows = pl.ds(pl.multiple_of(b * step, step), step)
            xhat, r = norm_parts(x_ref[rows, :].astype(F32))
            da1 = da1_ref[rows, :]
            sums_ref[0:1, :] += jnp.sum(da1 * xhat, 0, keepdims=True)
            sums_ref[1:2, :] += jnp.sum(da1, 0, keepdims=True)
            dg = da1 * rows_ref[0:1, :]
            dv = r * (
                dg
                - jnp.mean(dg, -1, keepdims=True)
                - xhat * jnp.mean(dg * xhat, -1, keepdims=True)
            )
            xg_ref[rows, :] = (dh1_ref[rows, :] + dv).astype(BF16)


def whole(*shape):
    return pl.BlockSpec(shape, lambda t: (0,) * len(shape))


def group(*shape):
    return pl.BlockSpec((1,) + shape, lambda t: (t,) + (0,) * len(shape))


def shaped(dtype, *shape):
    return jax.ShapeDtypeStruct(shape, dtype)


SMEM_WHOLE = pl.BlockSpec(memory_space=pltpu.SMEM)


def run_attention_forward(length, x, g0, rows, bqv):
    n = x.shape[0]
    groups, _, _, width = g0.shape
    heads = width // HEAD_DIM
    return pl.pallas_call(
        attention_forward,
        grid=(groups,),
        in_specs=[SMEM_WHOLE, whole(n, D), group(4, D, width), whole(16, D), group(2, width)],
        out_specs=[
            group(n, width), group(n, width), group(width, n), group(heads, n, n),
            group(n, width), whole(D, n), whole(n, D), whole(n, D), whole(D, n),
        ],
        out_shape=[
            shaped(BF16, groups, n, width), shaped(BF16, groups, n, width),
            shaped(BF16, groups, width, n), shaped(BF16, groups, heads, n, n),
            shaped(BF16, groups, n, width), shaped(BF16, D, n), shaped(F32, n, D),
            shaped(BF16, n, D), shaped(BF16, D, n),
        ],
        scratch_shapes=[
            pltpu.VMEM((n, D), BF16), pltpu.VMEM((n, width), BF16),
            pltpu.VMEM((width, n), BF16), pltpu.VMEM((width, n), BF16),
            pltpu.VMEM((n, D), F32),
        ],
        compiler_params=pltpu.CompilerParams(vmem_limit_bytes=VMEM_LIMIT),
        name="attention_forward",
    )(length, x, g0, rows, bqv)


def run_feed_forward(length, cot, a2, a2t, h1, g1, g2, rows):
    n = cot.shape[0]
    groups, _, width = g1.shape
    return pl.pallas_call(
        feed_forward_both,
        grid=(groups,),
        in_specs=[
            SMEM_WHOLE, whole(n, D), whole(n, D), whole(D, n), whole(n, D),
            group(D, width), group(D, width), whole(16, D),
        ],
        out_specs=[
            whole(n, D), group(D, width), group(D, width), whole(n, D), whole(n, D),
            whole(D, n), whole(16, D),
        ],
        out_shape=[
            shaped(BF16, n, D), shaped(BF16, groups, D, width), shaped(BF16, groups, D, width),
            shaped(F32, n, D), shaped(BF16, n, D), shaped(BF16, D, n), shaped(F32, 16, D),
        ],
        scratch_shapes=[
            pltpu.VMEM((n, D), BF16), pltpu.VMEM((D, n), BF16), pltpu.VMEM((n, D), F32),
            pltpu.VMEM((n, D), F32), pltpu.VMEM((n, width), BF16), pltpu.VMEM((n, width), BF16),
        ],
        compiler_params=pltpu.CompilerParams(vmem_limit_bytes=VMEM_LIMIT),
        name="feed_forward_both",
    )(length, cot, a2, a2t, h1, g1, g2, rows)


def run_attention_backward(x, g0, rows, dh1, gb, gbt, q, v, kt, p, o, a1t):
    n = x.shape[0]
    groups, _, _, width = g0.shape
    heads = width // HEAD_DIM
    return pl.pallas_call(
        attention_backward,
        grid=(groups,),
        in_specs=[
            whole(n, D), group(4, D, width), whole(16, D), whole(n, D), whole(n, D),
            whole(D, n), group(n, width), group(n, width), group(width, n),
            group(heads, n, n), group(n, width), whole(D, n),
        ],
        out_specs=[group(4, D, width), whole(n, D), whole(8, D), group(8, width)],
        out_shape=[
            shaped(BF16, groups, 4, D, width), shaped(BF16, n, D), shaped(F32, 8, D),
            shaped(F32, groups, 8, width),
        ],
        scratch_shapes=[
            pltpu.VMEM((n, width), BF16), pltpu.VMEM((16, n), F32), pltpu.VMEM((width, n), F32),
            pltpu.VMEM((n, width), BF16), pltpu.VMEM((n, width), BF16),
            pltpu.VMEM((n, width), BF16), pltpu.VMEM((n, D), F32),
        ],
        compiler_params=pltpu.CompilerParams(vmem_limit_bytes=VMEM_LIMIT),
        name="attention_backward",
    )(x, g0, rows, dh1, gb, gbt, q, v, kt, p, o, a1t)


Z_DEV, Y_DEV, X_DEV, C_DEV = 4, 2, 2, 2


class Place:
    def __init__(self):
        dp, self.t = lax.axis_index("dp"), lax.axis_index("tensor")
        self.dp = dp
        self.z, self.y = dp // 2, dp % 2
        self.x, self.c = self.t // 2, self.t % 2
        self.other_y = 1 - self.y
        self.zs = [
            self.z,
            self.z + 1 - 2 * (self.z % 2),
            self.z + 2 - 4 * (self.z // 2),
            3 - self.z,
        ]
        self.ts = [
            self.t,
            self.t + 1 - 2 * (self.t % 2),
            self.t + 2 - 4 * (self.t // 2),
            3 - self.t,
        ]
        self.to_z = [dict(dp=z * 2 + self.y) for z in self.zs]
        self.to_y = dict(dp=self.z * 2 + self.other_y)
        self.to_x = dict(tensor=self.ts[2])
        self.same_t = self.to_z[1:] + [dict(dp=z * 2 + self.other_y) for z in self.zs]
        self.same_dp = [dict(tensor=t) for t in self.ts[1:]]
        self.to_core = dict(tensor=self.ts[1])

    def group(self, k):
        return lax.select(
            k == 0, self.ts[0],
            lax.select(k == 1, self.ts[1], lax.select(k == 2, self.ts[2], self.ts[3])),
        )

    def greet(self, others=None):
        barrier = pltpu.get_barrier_semaphore()
        others = others or self.to_z[1:] + [self.to_y, self.to_x, self.to_core]
        for device in others:
            pl.semaphore_signal(
                barrier, inc=1, device_id=device, device_id_type=pl.DeviceIdType.MESH
            )
        pl.semaphore_wait(barrier, len(others))


class Links:
    def __init__(self, send_sem, recv_sem):
        self.send_sem, self.recv_sem = send_sem, recv_sem
        self.copies = []

    def add(self, device, src, dst):
        number = len(self.copies)
        copy = pltpu.make_async_remote_copy(
            src_ref=src,
            dst_ref=dst,
            send_sem=self.send_sem.at[number],
            recv_sem=self.recv_sem.at[number],
            device_id=device,
            device_id_type=pl.DeviceIdType.MESH,
        )
        self.copies.append(copy)
        return copy

    def sent(self, *apart):
        for copy in self.copies:
            if all(copy is not other for other in apart):
                copy.wait_send()


def flat(copies):
    for item in copies:
        if isinstance(item, list):
            yield from flat(item)
        else:
            yield item


def start(*copies):
    for copy in flat(copies):
        copy.start()


def recv(*copies):
    for copy in flat(copies):
        copy.wait_recv()


class Gather:
    def __init__(self, links, place, own, full, order, single=True, last=True):
        every = slice(None)
        y, other = place.y, place.other_y

        def same(device, k, yy, to):
            return links.add(device, full(k, every, yy), full(to, every, yy))

        def along_z(k, yy, block):
            here, passed = full(k, place.z, yy), full(k, place.zs[2], yy)
            return [
                links.add(place.to_z[1], block, here),
                links.add(place.to_z[2], block, here),
                links.add(place.to_z[1], passed, passed),
            ]

        self.z = along_z(0, y, own)
        if order == X_Z_Y:
            self.first = [links.add(place.to_x, own, full(2, place.z, y))]
            self.far = along_z(2, y, full(2, place.z, y))
            blocks = [(0, y), (2, y), (0, other), (2, other)]
        else:
            blocks = [(0, y), (0, other), (2, y), (2, other)]
        if order == Y_Z_X:
            self.first = [links.add(place.to_y, own, full(0, place.z, y))]
            self.far = along_z(0, other, full(0, place.z, other))
        if order == Z_Y_X and single:
            self.first = [same(place.to_y, 0, y, 0)]
        if order == Z_Y_X and not single:
            self.first = [links.add(place.to_y, own, full(0, place.z, y))]
            for k in range(1, 4):
                block = full(0, place.zs[k], y)
                self.first.append(links.add(place.to_y, block, block))
        self.second = [
            same(place.to_y, k, yy, k) if order == X_Z_Y else same(place.to_x, k, yy, 2)
            for k, yy in blocks[: 2 if last else 1]
        ]
        if not last:
            blocks = [block for block in blocks if block[0] == 0]
        self.core = [same(place.to_core, k, yy, k + 1) for k, yy in blocks]


Z_Y_X, Y_Z_X, X_Z_Y = range(3)


def fused_forward(
    tie_ref, len_ref, tokens_ref, gains_ref, bias_ref, in_ref, out_ref, expand_ref,
    project_ref,
    gq_ref, gw_ref, flat1_ref, flat2_ref, rows_ref,
    q_ref, v_ref, kt_ref, p_ref, scale_ref, o_ref, a1t_out, h1_out, a2_out, a2t_out,
    own0_ref, ownw_ref, own1_ref, own2_ref, square_ref, vec_ref,
    all0_ref, allw_ref, w1_ref, w2_ref, vecs_ref, bqv_ref, x_ref, a1_ref, k_ref, qa_ref, vt_ref, ot_ref, a1t_ref, h1_ref, a2_ref, a2t_ref,
    send_sem, recv_sem, local_sem, flush_sem, row_sem,
):
    t = pl.program_id(0)
    n, _ = x_ref.shape
    width = allw_ref.shape[-1]
    heads = width // HEAD_DIM
    step = 256
    place = Place()
    length = len_ref[place.t]
    links = Links(send_sem, recv_sem)
    z, y, x, c = place.z, place.y, place.x, place.c
    mine_there = vecs_ref.at[z, y, x, c]
    column = vecs_ref.at[:, :, x, c]
    vec_one = [links.add(device, vec_ref, mine_there) for device in place.same_t]
    vec_two = [links.add(device, column, column) for device in place.same_dp]
    seg0 = Gather(
        links, place, own0_ref, lambda k, z, y: all0_ref.at[k, z, y], Z_Y_X, single=False
    )
    segw = Gather(links, place, ownw_ref, lambda k, z, y: allw_ref.at[k, z, y], Z_Y_X)
    seg1 = Gather(
        links, place, own1_ref, lambda k, z, y: w1_ref.at[k, z, y], Y_Z_X, last=False
    )
    seg2 = Gather(
        links, place, own2_ref, lambda k, z, y: w2_ref.at[k, z, y], X_Z_Y, last=False
    )
    flush = [
        [
            pltpu.make_async_copy(ref.at[k], flat.at[k], flush_sem.at[i, k])
            for k in range(3)
        ]
        for i, (ref, flat) in enumerate([(w1_ref, flat1_ref), (w2_ref, flat2_ref)])
    ]
    put_a1t = pltpu.make_async_copy(a1t_ref, a1t_out, local_sem.at[0])
    put_a2t = pltpu.make_async_copy(a2t_ref, a2t_out, local_sem.at[1])
    puts = []
    for i in range(n // step):
        rows = pl.ds(i * step, step)
        puts.append([
            pltpu.make_async_copy(h1_ref.at[rows], h1_out.at[rows], row_sem.at[0, i]),
            pltpu.make_async_copy(a2_ref.at[rows], a2_out.at[rows], row_sem.at[1, i]),
        ])
    fetch = pltpu.make_async_copy(tokens_ref.at[place.t], x_ref, local_sem.at[2])

    def relay_z(copies):
        recv(copies[1])
        start(copies[2])

    def pass_own(seg):
        recv(seg.z[0], seg.z[2])
        if seg is segw:
            start(seg.first)
        start(seg.second[0], seg.core[0])

    def pass_second(seg):
        recv(seg.second)
        if seg is seg2:
            start(seg.core[1])

    def pass_first(seg):
        recv(seg.first)
        if seg is segw:
            start(seg.second[1], seg.core[1])
        else:
            start(seg.far[1], seg.far[0])

    def pass_far(seg):
        recv(seg.far[0], seg.far[2])
        start(seg.core[1:] if seg is seg1 else [])

    def pass_core(seg, i):
        recv(seg.second[i])
        start(seg.core[2 + i])

    plan = [
        (0, 0, lambda: (pass_own(segw), pass_first(seg1), relay_z(seg2.z), pass_first(seg2))),
        (0, 3, lambda: (pass_first(segw), relay_z(seg1.z), pass_core(seg0, 0))),
        (1, 0, lambda: recv(seg0.core[:2])),
        (1, 1, lambda: relay_z(seg1.far)),
        (1, 3, lambda: pass_core(seg0, 1)),
        (1, 4, lambda: (recv(segw.core[:2]), pass_core(segw, 0), pass_own(seg2))),
        (2, 1, lambda: relay_z(seg2.far)),
        (2, 2, lambda: pass_core(segw, 1)),
        (2, 3, lambda: pass_own(seg1)),
        (3, 0, lambda: (recv(seg0.core[2:]), pass_far(seg1), flush[0][0].start())),
        (3, 2, lambda: (pass_second(seg2), flush[1][0].start())),
        (3, 3, lambda: (pass_far(seg2), flush[1][2].start())),
        (3, 4, lambda: recv(segw.core[2:])),
    ]

    def serve(point, head=None):
        for step, where, act in plan:
            if head is not None and where >= 2:
                pl.when((t == step) & (head == where - 2))(lambda act=act: (act(), None)[1])
            elif where == point:
                pl.when(t == step)(lambda act=act: (act(), None)[1])

    @pl.when(t == 0)
    def _():
        s0, s1, s2, s3 = tie_ref[0], tie_ref[1], tie_ref[2], tie_ref[3]
        fetch.start()
        square_ref[...] = jnp.zeros_like(square_ref)
        gain = gains_ref.shape[-1]
        square_ref[0:1, :gain] = gains_ref[s0].astype(F32)[0:1]
        square_ref[1:2, :gain] = gains_ref[s2].astype(F32)[1:2]
        kinds = [s0, s0, s0, s1, s2, s3, s2, s2, s2, s2]
        for i, source in enumerate(kinds):
            wide = bias_ref[i].astype(F32)
            here = lax.broadcasted_iota(jnp.int32, wide.shape, 0) == source
            square_ref[2 + i : 3 + i, :gain] = jnp.sum(
                jnp.where(here, wide, 0.0), 0, keepdims=True
            )
        vec_ref[...] = square_ref[...].T[:gain]
        for j in range(3):
            own0_ref[:, j * width : (j + 1) * width] = in_ref[s0, j]
        place.greet(place.same_t + place.same_dp)
        start(vec_one, seg0.z[1], seg0.z[0], seg0.first[0])
        vecs_ref[z, y, x, c] = vec_ref[...]
        ones = lax.broadcasted_iota(jnp.int32, (vt_ref.shape[1] - HEAD_DIM, n), 0) == 0
        for h in range(heads):
            vt_ref[h, HEAD_DIM:, :] = ones.astype(BF16)
        all0_ref[0, z, y] = own0_ref[...]
        ownw_ref[...] = out_ref[s1].T
        allw_ref[0, z, y] = ownw_ref[...]
        own1_ref[...] = expand_ref[s2]
        own2_ref[...] = project_ref[s3]
        w1_ref[0, z, y] = own1_ref[...]
        w2_ref[0, z, y] = own2_ref[...]
        recv(vec_one)
        start(vec_two)
        relay_z(seg0.z)
        start(seg0.first[2])
        recv(seg0.z[0])
        start(seg0.first[1], segw.z[1], segw.z[0], seg2.z[1])
        recv(vec_two)
        start(seg2.first)
        vecs = vecs_ref[...].reshape(D, vecs_ref.shape[-1]).T[:16]
        rows_ref[...] = vecs
        recv(seg0.z[2])
        start(seg0.first[3], seg1.first, seg0.second[0], seg0.core[0])
        for k in range(4):
            part = slice(k * width, (k + 1) * width)
            bqv_ref[k, 0:1, :width] = vecs[3:4, part]
            bqv_ref[k, 0:1, width : 2 * width] = jnp.zeros((1, width), F32)
            bqv_ref[k, 0:1, 2 * width :] = vecs[4:5, part]
        fetch.wait()

        @pl.loop(0, n // step)
        def _(b):
            rows = pl.ds(pl.multiple_of(b * step, step), step)
            wide = x_ref[rows, :].astype(F32)
            xhat, _ = norm_parts(wide)
            a1 = (xhat * rows_ref[0:1, :] + rows_ref[2:3, :]).astype(BF16)
            a1_ref[rows, :] = a1
            a1t_ref[:, rows] = a1.T
            h1_ref[rows, :] = wide + rows_ref[5:6, :]

        put_a1t.start()
        relay_z(segw.z)
        start(seg2.z[0], seg1.z[1], seg1.z[0])
        recv(seg0.first)
        start(seg0.second[1], seg0.core[1])

    serve(0)
    gq = all0_ref[t].reshape(D, 3 * width)
    gq_ref[0] = gq
    mine = place.group(t)
    qkv = dot_nn(a1_ref[...], gq) + bqv_ref[mine, 0:1, :]
    q = qkv[:, :width].astype(BF16) * jnp.asarray(HEAD_DIM ** -0.5, BF16)
    k = qkv[:, width : 2 * width].astype(BF16)
    v = qkv[:, 2 * width :].astype(BF16)
    q_ref[0] = q
    kt_ref[0] = k.T
    v_ref[0] = v
    vt = v.T
    for h in range(heads):
        vt_ref[h, :HEAD_DIM, :] = vt[h * HEAD_DIM : (h + 1) * HEAD_DIM]
    spare = k_ref.shape[1] - width
    dead = lax.broadcasted_iota(jnp.int32, (n, spare), 0) >= length
    first_column = lax.broadcasted_iota(jnp.int32, (n, spare), 1) == 0
    k_ref[:, :width] = k
    k_ref[:, width:] = jnp.where(first_column & dead, MASKED, 0.0).astype(BF16)
    qa_ref[:, :width] = q
    qa_ref[:, width:] = jnp.where(first_column, 1.0, 0.0).astype(BF16)

    serve(1)
    scale_ref[0, heads:, :] = jnp.zeros((scale_ref.shape[1] - heads, n), F32)
    @pl.loop(0, heads)
    def _(h):
        lane = lax.broadcasted_iota(jnp.int32, (1, qa_ref.shape[1]), 1)
        keep = ((lane >= h * HEAD_DIM) & (lane < (h + 1) * HEAD_DIM)) | (lane >= width)
        key = lax.broadcasted_iota(jnp.int32, (step, step), 0)
        query = lax.broadcasted_iota(jnp.int32, (step, step), 1)
        head = pl.ds(pl.multiple_of(h * HEAD_DIM, HEAD_DIM), HEAD_DIM)

        def scores(b):
            first, last = b * step, (b + 1) * step
            q = jnp.where(keep, qa_ref[first:last, :], jnp.zeros((), BF16))
            return dot_nt(k_ref[:last, :], q)

        def attend(b, s):
            first, last = b * step, (b + 1) * step
            near = jnp.where(key <= query, s[first:], MASKED)
            top = jnp.max(near, 0, keepdims=True)
            if b:
                far = s[:first]
                top = jnp.maximum(top, jnp.max(far, 0, keepdims=True))
            e_near = jnp.exp((near - top).astype(BF16))
            p_ref[0, h, first:last, first:last] = e_near
            o = dot_nn(vt_ref[h, :, first:last], e_near)
            if b:
                e_far = jnp.exp((far - top).astype(BF16))
                p_ref[0, h, :first, first:last] = e_far
                o += dot_nn(vt_ref[h, :, :first], e_far)
            scale = 1.0 / o[HEAD_DIM : HEAD_DIM + 1]
            scale_ref[0, pl.ds(h, 1), first:last] = scale
            ot_ref[head, first:last] = (o[:HEAD_DIM] * scale).astype(BF16)

        s = scores(0)
        for b in range(n // step):
            ahead = scores(b + 1) if b + 1 < n // step else None
            attend(b, s)
            s = ahead
        serve(2, h)

    gw_ref[0] = allw_ref[t].reshape(gw_ref.shape[1:])
    o = ot_ref[...].T
    o_ref[0] = o
    h1_ref[...] += dot_nt(o, gw_ref[0])

    @pl.when(t == 3)
    def _():
        for i, rows in enumerate(blocks(n, step)):
            xhat, _ = norm_parts(h1_ref[rows, :])
            a2 = (xhat * rows_ref[1:2, :] + rows_ref[6:7, :]).astype(BF16)
            a2_ref[rows, :] = a2
            a2t_ref[:, rows] = a2.T
            for put in puts[i]:
                put.start()
        put_a2t.start()
        recv(seg2.core)
        flush[1][1].start()
        recv(seg1.core)
        flush[0][1].start()
        pass_second(seg1)
        flush[0][2].start()
        links.sent()
        for copies in flush + puts + [[put_a1t, put_a2t]]:
            for copy in copies:
                copy.wait()


N_GATHER = 10 + 13 + 10 + 10 + 10
VMEM_WHOLE = pl.BlockSpec(memory_space=pltpu.VMEM)
ANY_WHOLE = pl.BlockSpec(memory_space=pl.ANY)


def run_fused_forward(tie, lengths, tokens, gains, biases, w_in, w_out, w_expand, w_project):
    groups, n, _ = tokens.shape
    depth, width = w_in.shape[-2:]
    heads = width // HEAD_DIM
    hidden = w_expand.shape[-1]
    w_project = w_project.transpose(0, 2, 1)
    biases = biases.transpose(1, 0, 2)
    own = gains.shape[-1]
    return pl.pallas_call(
        fused_forward,
        grid=(groups,),
        in_specs=[SMEM_WHOLE, SMEM_WHOLE, ANY_WHOLE] + [VMEM_WHOLE] * 6,
        out_specs=[
            group(D, 3 * width), group(D, width), ANY_WHOLE, ANY_WHOLE, VMEM_WHOLE,
            group(n, width), group(n, width), group(width, n), group(heads, n, n),
            group(8, n), group(n, width), ANY_WHOLE, ANY_WHOLE, ANY_WHOLE, ANY_WHOLE,
        ],
        out_shape=[
            shaped(BF16, groups, D, 3 * width), shaped(BF16, groups, D, width),
            shaped(BF16, groups, Z_DEV, Y_DEV, depth, hidden),
            shaped(BF16, groups, Z_DEV, Y_DEV, depth, hidden),
            shaped(F32, 16, D),
            shaped(BF16, groups, n, width), shaped(BF16, groups, n, width),
            shaped(BF16, groups, width, n), shaped(BF16, groups, heads, n, n),
            shaped(F32, groups, 8, n), shaped(BF16, groups, n, width), shaped(BF16, D, n), shaped(F32, n, D),
            shaped(BF16, n, D), shaped(BF16, D, n),
        ],
        scratch_shapes=[
            pltpu.VMEM((depth, 3 * width), BF16), pltpu.VMEM((depth, width), BF16),
            pltpu.VMEM((depth, hidden), BF16), pltpu.VMEM((depth, hidden), BF16),
            pltpu.VMEM((128, 128), F32), pltpu.VMEM((own, 128), F32),
            pltpu.VMEM((groups, Z_DEV, Y_DEV, depth, 3 * width), BF16),
            pltpu.VMEM((groups, Z_DEV, Y_DEV, depth, width), BF16),
            pltpu.VMEM((groups, Z_DEV, Y_DEV, depth, hidden), BF16),
            pltpu.VMEM((groups, Z_DEV, Y_DEV, depth, hidden), BF16),
            pltpu.VMEM((Z_DEV, Y_DEV, X_DEV, C_DEV, own, 128), F32),
            pltpu.VMEM((groups, 8, 3 * width), F32),
            pltpu.VMEM((n, D), BF16), pltpu.VMEM((n, D), BF16), pltpu.VMEM((n, 256), BF16),
            pltpu.VMEM((n, 256), BF16), pltpu.VMEM((heads, HEAD_DIM + 16, n), BF16),
            pltpu.VMEM((width, n), BF16),
            pltpu.VMEM((D, n), BF16), pltpu.VMEM((n, D), F32), pltpu.VMEM((n, D), BF16),
            pltpu.VMEM((D, n), BF16),
            pltpu.SemaphoreType.DMA((N_GATHER,)), pltpu.SemaphoreType.DMA((N_GATHER,)),
            pltpu.SemaphoreType.DMA((3,)), pltpu.SemaphoreType.DMA((2, 4)),
            pltpu.SemaphoreType.DMA((2, n // 256)),
        ],
        compiler_params=pltpu.CompilerParams(
            vmem_limit_bytes=VMEM_LIMIT, collective_id=0, has_side_effects=True
        ),
        name="fused_forward",
    )(tie, lengths, tokens, gains, biases, w_in, w_out, w_expand, w_project)


class Result:
    def __init__(self, links, place, own_ref, passing_ref, out_ref, step, sem, count):
        self.x, self.core, self.far, self.keep, self.keep_far = [], [], [], [], []
        for i in range(count):
            rows = pl.ds(i * step, step)
            mine, theirs = out_ref.at[place.t, rows], out_ref.at[place.ts[2], rows]
            own, passing = own_ref.at[rows], passing_ref.at[rows]
            self.x.append(links.add(place.to_x, own, passing))
            self.core.append(links.add(place.to_core, own, mine))
            self.far.append(links.add(place.to_core, passing, theirs))
            self.keep.append(pltpu.make_async_copy(own, mine, sem.at[0, i]))
            self.keep_far.append(pltpu.make_async_copy(passing, theirs, sem.at[1, i]))

    def send(self, i):
        start(self.x[i], self.core[i], self.keep[i])

    def pass_on(self, i):
        recv(self.x[i])
        start(self.far[i], self.keep_far[i])

    def finish(self):
        recv(self.core, self.far)
        for copy in self.keep + self.keep_far:
            copy.wait()


def low(value):
    return jnp.asarray(value, BF16)


def pair_order(i):
    return i + 1 - 2 * (i % 2)


def fused_feed_forward(
    len_ref, cot_ref, a2_ref, a2t_in, h1_in, far1_ref, far2_ref, rows_ref,
    out_out, fold_ref, work_out, dh1_out, gb_out, gbt_out, sums_ref,
    gf_ref, gft_ref, feed_ref, da2_ref, h_ref, df_ref, weights_ref, missing_ref, third_ref,
    stage_ref, land_ref, near_ref, cross_ref, a2t_ref, h1_ref, out_ref, work_ref,
    send_sem, recv_sem, local_sem, row_sem,
):
    t = pl.program_id(0)
    n = gf_ref.shape[0]
    step = 256
    depth = stage_ref.shape[-2]
    place = Place()
    length = len_ref[place.t]
    links = Links(send_sem, recv_sem)
    y, other = place.y, place.other_y
    last = [
        links.add(place.to_x, far1_ref.at[0, :, other], missing_ref.at[0, 0]),
        links.add(place.to_y, far2_ref.at[2, :, y], missing_ref.at[1, 0]),
    ]
    last_core = [
        links.add(place.to_core, missing_ref.at[i, 0], missing_ref.at[i, 1]) for i in range(2)
    ]
    third = [
        links.add(place.to_core, far_ref.at[2, :, y], third_ref.at[i])
        for i, far_ref in enumerate([far1_ref, far2_ref])
    ]
    core = [
        [links.add(place.to_core, stage_ref.at[i], land_ref.at[s, i]) for i in range(2)]
        for s in range(2)
    ]
    cross = [
        links.add(place.to_y, near_ref.at[i, :, other], cross_ref.at[i]) for i in range(2)
    ]
    fetch = pltpu.make_async_copy(cot_ref.at[place.t], gf_ref, local_sem.at[0])
    gb_ref, gbt_ref, dh1_ref = gf_ref, gft_ref, da2_ref
    late = [
        pltpu.make_async_copy(a2t_in, a2t_ref, local_sem.at[5]),
        pltpu.make_async_copy(h1_in, h1_ref, local_sem.at[6]),
    ]
    puts = []
    for i in range(n // step):
        rows = pl.ds(i * step, step)
        puts.append([
            pltpu.make_async_copy(ref.at[rows], out.at[rows], row_sem.at[j, i])
            for j, (ref, out) in enumerate(
                [(out_ref, out_out), (dh1_ref, dh1_out), (gb_ref, gb_out)]
            )
        ])
    put_gbt = pltpu.make_async_copy(gbt_ref, gbt_out, local_sem.at[7])
    put_work = pltpu.make_async_copy(work_ref, work_out, local_sem.at[8])
    k = pair_order(t)
    mine = place.group(k)

    def load(step, whole, slot):
        for i, far_ref in enumerate([far1_ref, far2_ref]):
            group = far_ref.at[pair_order(step)]
            to = weights_ref.at[slot, i]
            if not whole:
                group, to = group.at[:, y], to.at[:, y]
            yield pltpu.make_async_copy(group, to, local_sem.at[1 + 2 * slot + i])

    def live_rows(b):
        at = b * step + lax.broadcasted_iota(jnp.int32, (step, 1), 0)
        return (at < length).astype(F32)

    @pl.when(t == 0)
    def _():
        fetch.start()
        for copy in load(0, True, 0):
            copy.start()
        for copy in late:
            copy.start()
        place.greet()
        start(last, third)
        sums_ref[...] = jnp.zeros_like(sums_ref)
        feed_ref[...] = jnp.zeros_like(feed_ref)
        da2_ref[...] = jnp.zeros_like(da2_ref)
        fetch.wait()

        @pl.loop(0, n // step)
        def _(b):
            rows = pl.ds(pl.multiple_of(b * step, step), step)
            g = (gf_ref[rows, :].astype(F32) * live_rows(b)).astype(BF16)
            gf_ref[rows, :] = g
            gft_ref[:, rows] = g.T
            sums_ref[7:8, :] += jnp.sum(g.astype(F32), 0, keepdims=True)

    for i in range(4):
        @pl.when(t == i)
        def _():
            if i == 2:
                recv(last_core, third)
            else:
                for copy in load(i, i < 2, i % 2):
                    copy.wait()
            if i in (0, 2):
                for copy in load(i + 1, i + 1 < 2, (i + 1) % 2):
                    copy.start()
            for j in range(2):
                if i == 2:
                    weights_ref[0, j, :, y] = third_ref[j]
                if i >= 2:
                    weights_ref[i % 2, j, :, other] = missing_ref[j, 3 - i]

    bias = rows_ref[pl.ds(8 + mine, 1), :]
    w1 = weights_ref[t % 2, 0].reshape(D, -1)
    w2 = weights_ref[t % 2, 1].reshape(D, -1)
    @pl.loop(0, n // step)
    def _(b):
        rows = pl.ds(pl.multiple_of(b * step, step), step)
        f = (dot_nn(a2_ref[rows, :], w1) + bias).astype(BF16)
        dh = dot_nn(gf_ref[rows, :], w2)
        f2 = f * f
        th = jnp.tanh(f * (low(SQRT_2_PI) + low(SQRT_2_PI * 0.044715) * f2))
        half = low(0.5) + low(0.5) * th
        h = f * half
        slope = half + f * (low(0.5) - low(0.5) * th * th) * (
            low(SQRT_2_PI) + low(3 * SQRT_2_PI * 0.044715) * f2
        )
        df = (dh * slope.astype(F32)).astype(BF16)
        h_ref[rows, :] = h
        df_ref[rows, :] = df
        sums_ref[pl.ds(8 + mine, 1), :] += jnp.sum(df.astype(F32), 0, keepdims=True)
        feed_ref[rows, :] += dot_nt(h, w2)
        da2_ref[rows, :] += dot_nt(df, w1)

    @pl.when(t == 1)
    def _():
        recv(last)
        start(last_core)

    @pl.when(t == 0)
    def _():
        late[0].wait()

    def put(ref):
        @pl.loop(0, Z_DEV)
        def _(z):
            rows = pl.ds(pl.multiple_of(z * Y_DEV * depth, Y_DEV * depth), Y_DEV * depth)
            for i, (left_ref, right_ref) in enumerate([(a2t_ref, df_ref), (gft_ref, h_ref)]):
                value = dot_nn(left_ref[rows, :], right_ref[...])
                ref[i, z] = value.reshape(Y_DEV, depth, value.shape[-1]).astype(BF16)

    def reduced(ref):
        return lambda i, s, z: (
            ref[i, z].astype(F32) + land_ref[s, i, z].astype(F32)
        ).astype(BF16)

    @pl.when(t == 0)
    def _():
        put(stage_ref)
        start(core[0])

    @pl.when(t == 1)
    def _():
        put(near_ref)
        recv(core[0])

        @pl.loop(0, Z_DEV)
        def _(z):
            for i in range(2):
                near_ref[i, z] = reduced(near_ref)(i, 0, z)

        start(cross)

    @pl.when(t == 2)
    def _():
        for copy in core[0]:
            copy.wait_send()
        put(stage_ref)
        start(core[1])

    @pl.when(t == 3)
    def _():
        put(work_ref)
        late[1].wait()
        for i, rows in enumerate(blocks(n, step)):
            live = live_rows(i)
            h1 = h1_ref[rows, :]
            out_ref[rows, :] = (live * (h1 + (feed_ref[rows, :] + rows_ref[7:8, :]))).astype(BF16)
            xhat, r = norm_parts(h1)
            da2 = da2_ref[rows, :]
            sums_ref[1:2, :] += jnp.sum(da2 * xhat, 0, keepdims=True)
            sums_ref[6:7, :] += jnp.sum(da2, 0, keepdims=True)
            dg = da2 * rows_ref[1:2, :]
            dv = r * (
                dg
                - jnp.mean(dg, -1, keepdims=True)
                - xhat * jnp.mean(dg * xhat, -1, keepdims=True)
            )
            dh1 = gf_ref[rows, :].astype(F32) + dv
            dh1_ref[rows, :] = dh1
            gb = dh1.astype(BF16)
            gb_ref[rows, :] = gb
            gbt_ref[:, rows] = gb.T
            sums_ref[5:6, :] += jnp.sum(gb.astype(F32), 0, keepdims=True)
            for copy in puts[i]:
                copy.start()
        put_gbt.start()
        recv(core[1])

        @pl.loop(0, Z_DEV)
        def _(z):
            for i in range(2):
                work_ref[i, z] = reduced(work_ref)(i, 1, z)

        put_work.start()
        recv(cross)

        @pl.loop(0, Z_DEV)
        def _(z):
            for i in range(2):
                fold_ref[i, z] = (
                    near_ref[i, z, y].astype(F32) + cross_ref[i, z].astype(F32)
                ).astype(BF16)

        links.sent(*core[0])
        for copies in puts + [[put_gbt, put_work]]:
            for copy in copies:
                copy.wait()


def run_fused_feed_forward(lengths, cot, a2, a2t, h1, g1, g2, rows):
    n = cot.shape[1]
    groups, _, _, depth, hidden = g1.shape
    both = (2, Z_DEV, Y_DEV, depth, hidden)
    fold = (2, Z_DEV, depth, hidden)
    return pl.pallas_call(
        fused_feed_forward,
        grid=(groups,),
        in_specs=[SMEM_WHOLE, ANY_WHOLE, VMEM_WHOLE] + [ANY_WHOLE] * 4 + [VMEM_WHOLE],
        out_specs=[ANY_WHOLE, VMEM_WHOLE] + [ANY_WHOLE] * 4 + [VMEM_WHOLE],
        out_shape=[
            shaped(BF16, n, D), shaped(BF16, *fold), shaped(BF16, *both), shaped(F32, n, D),
            shaped(BF16, n, D), shaped(BF16, D, n), shaped(F32, 16, D),
        ],
        scratch_shapes=[
            pltpu.VMEM((n, D), BF16), pltpu.VMEM((D, n), BF16), pltpu.VMEM((n, D), F32),
            pltpu.VMEM((n, D), F32), pltpu.VMEM((n, hidden), BF16), pltpu.VMEM((n, hidden), BF16),
            pltpu.VMEM((2,) + both, BF16),
            pltpu.VMEM((2,) + fold, BF16), pltpu.VMEM(fold, BF16), pltpu.VMEM(both, BF16),
            pltpu.VMEM((2,) + both, BF16),
            pltpu.VMEM(both, BF16), pltpu.VMEM(fold, BF16),
            pltpu.VMEM((D, n), BF16), pltpu.VMEM((n, D), F32), pltpu.VMEM((n, D), BF16),
            pltpu.VMEM(both, BF16),
            pltpu.SemaphoreType.DMA((12,)), pltpu.SemaphoreType.DMA((12,)),
            pltpu.SemaphoreType.DMA((9,)), pltpu.SemaphoreType.DMA((3, n // 256)),
        ],
        compiler_params=pltpu.CompilerParams(
            vmem_limit_bytes=VMEM_LIMIT, collective_id=1, has_side_effects=True
        ),
        name="fused_feed_forward",
    )(lengths, cot, a2, a2t, h1, g1, g2, rows)
class Reduce:
    def __init__(
        self, links, place, work, acc, cross_ref, far_ref, mid_ref, last_ref, side_ref,
        slots=(0, 1), split=False,
    ):
        self.place, self.work, self.acc = place, work, acc
        self.cross_ref, self.far_ref, self.mid_ref = cross_ref, far_ref, mid_ref
        self.last_ref, self.side_ref = last_ref, side_ref
        self.two = len(slots) == 2
        zs = place.zs
        self.y = {
            s: [
                links.add(
                    place.to_y, work(s, zs[j], place.other_y),
                    cross_ref.at[s if self.two else 0, zs[j]],
                )
                for j in (1, 3, 2, 0)
            ]
            for s in slots
        }
        self.z = [
            [
                links.add(place.to_z[1], acc(s, zs[1]), far_ref.at[s, 0]),
                links.add(place.to_z[1], acc(s, zs[3]), far_ref.at[s, 1]),
                links.add(place.to_z[2], mid_ref.at[s, 1], far_ref.at[s, 2]),
            ]
            for s in range(1 if split else 2)
        ]
        self.x = links.add(place.to_x, last_ref, side_ref)

    def fold_y(self, s, half):
        for i, j in [(0, 1), (1, 3), (2, 2), (3, 0)][2 * half : 2 * half + 2]:
            z = self.place.zs[j]
            recv(self.y[s][i])
            value = self.work(s, z, self.place.y)[...].astype(F32)
            cross = self.cross_ref[s if self.two else 0, z].astype(F32)
            self.acc(s, z)[...] = (value + cross).astype(BF16)
            if i < 2:
                start(self.z[s][i])

    def fold_z(self, s):
        recv(self.z[s][:2])
        for i in (1, 0):
            value = self.acc(s, self.place.zs[2 * i])[...].astype(F32)
            self.mid_ref[s, i] = (value + self.far_ref[s, i].astype(F32)).astype(BF16)
            if i:
                start(self.z[s][2])

    def own(self, s):
        recv(self.z[s][2])
        return self.mid_ref[s, 0].astype(F32) + self.far_ref[s, 2].astype(F32)

    def send_x(self):
        self.last_ref[...] = self.own(1).astype(BF16)
        start(self.x)

    def total(self):
        value = self.own(0)
        recv(self.x)
        return value + self.side_ref[...].astype(F32)


class ReduceHalves:
    def __init__(self, links, place, work, landings, last_ref):
        self.place, self.work = place, work
        self.cross, self.far, self.mid, self.far2, self.mid2, self.fin2, self.cross2 = landings
        self.last_ref = last_ref
        zs, half = place.zs, last_ref.shape[0] // 2
        self.low, self.high = pl.ds(0, half), pl.ds(half, half)
        every = slice(None)
        y, other = place.y, place.other_y
        self.y = [
            links.add(place.to_y, work.at[zs[j], other, self.low], self.cross.at[zs[j]])
            for j in (1, 3, 2, 0)
        ]
        self.z = [
            links.add(place.to_z[1], work.at[zs[1], y, self.low], self.far.at[0]),
            links.add(place.to_z[1], work.at[zs[3], y, self.low], self.far.at[1]),
            links.add(place.to_z[2], self.mid.at[1], self.far.at[2]),
        ]
        self.z2 = [
            links.add(place.to_z[1], work.at[zs[1], every, self.high], self.far2.at[0]),
            links.add(place.to_z[1], work.at[zs[3], every, self.high], self.far2.at[1]),
            links.add(place.to_z[2], self.mid2.at[1], self.far2.at[2]),
        ]
        self.y2 = links.add(place.to_y, self.fin2.at[other], self.cross2)

    def begin(self):
        start(self.y, self.z2[:2])

    def add(self, target, left, right):
        target[...] = (left[...].astype(F32) + right[...].astype(F32)).astype(BF16)

    def fold_y(self):
        y, zs = self.place.y, self.place.zs
        for i, j in enumerate((1, 3, 2, 0)):
            recv(self.y[i])
            block = self.work.at[zs[j], y, self.low]
            self.add(block, block, self.cross.at[zs[j]])
            if i < 2:
                start(self.z[i])

    def fold_high(self):
        recv(self.z2[:2])
        for i in (1, 0):
            block = self.work.at[self.place.zs[2 * i], :, self.high]
            self.add(self.mid2.at[i], block, self.far2.at[i])
            if i:
                start(self.z2[2])

    def cross_high(self):
        recv(self.z2[2])
        self.add(self.fin2, self.mid2.at[0], self.far2.at[2])
        start(self.y2)

    def fold_z(self):
        recv(self.z[:2])
        for i in (1, 0):
            block = self.work.at[self.place.zs[2 * i], self.place.y, self.low]
            self.add(self.mid.at[i], block, self.far.at[i])
            if i:
                start(self.z[2])

    def finish(self):
        recv(self.z[2])
        self.add(self.last_ref.at[self.low], self.mid.at[0], self.far.at[2])
        recv(self.y2)
        self.add(self.last_ref.at[self.high], self.fin2.at[self.place.y], self.cross2)


def fused_backward(
    tokens_ref, gq_in, gw_in, rows_ref, dh1_ref, gb_ref, gbt_in, q_in, v_in, kt_in,
    p_ref, scale_in, o_in, a1t_in, layer_in, fold_in, work_in, early_ref,
    out_ref, layerout_ref, part0_ref, partw_ref, part1_ref, part2_ref, total_ref,
    gq_ref, gw_ref, q_ref, v_ref, kt_ref, scale_ref, o_ref,
    a1t_ref, gbt_ref, layer_ref, fold_ref, work_ref, do_ref, delta_ref, dqt_ref, dkv_ref, dqkv_ref, da1_ref, own_ref, passing_ref, passlayer_ref, bqv_ref,
    folded_ref, cross1_ref, far1_ref, mid1_ref, last1_ref, side1_ref,
    cross2_ref, far2_ref, mid2_ref, last2_ref, side2_ref,
    stagew_ref, landw_ref, workw_ref, crossw_ref, farw_ref, midw_ref, lastw_ref, sidew_ref,
    stage0_ref, land0_ref, work0_ref, cross0_ref, far0_ref, mid0_ref, last0_ref, side0_ref,
    sums_ref, sumland_ref,
    send_sem, recv_sem, local_sem, result_sem, group_sem, *tail_refs,
):
    t = pl.program_id(0)
    n = own_ref.shape[0]
    width = gw_ref.shape[-1]
    depth = part0_ref.shape[0]
    heads = width // HEAD_DIM
    step = n // 4
    place = Place()
    y = place.y
    links = Links(send_sem, recv_sem)
    k, i = group_and_block(t)
    mine = place.group(k)
    now = k % 2
    out = Result(links, place, own_ref, passing_ref, out_ref, step, result_sem.at[0], 4)
    layer = Result(links, place, layer_ref, passlayer_ref, layerout_ref, step, result_sem.at[1], 4)
    fetch = pltpu.make_async_copy(tokens_ref.at[place.t], own_ref, local_sem.at[0])
    fetch_layer, fetch_work, fetch_fold, fetch_gbt, fetch_a1t = [
        pltpu.make_async_copy(there, here, local_sem.at[1 + j])
        for j, (there, here) in enumerate([
            (layer_in, layer_ref), (work_in, work_ref), (fold_in, fold_ref),
            (gbt_in, gbt_ref), (a1t_in, a1t_ref),
        ])
    ]
    def operands(group):
        slot = group % 2
        pairs = [
            (gw_in, gw_ref), (scale_in, scale_ref), (o_in, o_ref), (v_in, v_ref),
            (q_in, q_ref), (kt_in, kt_ref), (gq_in, gq_ref),
        ]
        return [
            pltpu.make_async_copy(there.at[group], here.at[slot], group_sem.at[slot, j])
            for j, (there, here) in enumerate(pairs)
        ]

    corew = [links.add(place.to_core, stagew_ref, landw_ref.at[i]) for i in range(2)]
    core0 = [links.add(place.to_core, stage0_ref, land0_ref.at[i]) for i in range(2)]
    def half_done(i, *landing):
        return Reduce(
            links, place, lambda s, z, y: work_ref.at[i, z, y],
            lambda s, z: folded_ref.at[i, z] if s else fold_ref.at[i, z],
            *landing, slots=(1,),
        )

    seg1 = half_done(0, cross1_ref, far1_ref, mid1_ref, last1_ref, side1_ref)
    seg2 = half_done(1, cross2_ref, far2_ref, mid2_ref, last2_ref, side2_ref)
    segw = Reduce(
        links, place, lambda s, z, y: workw_ref.at[s, z, y],
        lambda s, z: workw_ref.at[s, z, y],
        crossw_ref, farw_ref, midw_ref, lastw_ref, sidew_ref,
    )
    seg0 = Reduce(
        links, place, lambda s, z, y: work0_ref.at[s, z, y],
        lambda s, z: work0_ref.at[s, z, y],
        cross0_ref, far0_ref, mid0_ref, last0_ref, side0_ref, slots=(0,), split=True,
    )
    tail = ReduceHalves(links, place, work0_ref.at[1], tail_refs, last0_ref)
    sum_core, sum_y, *sum_z, sum_x = [
        links.add(to, sums_ref.at[i], sumland_ref.at[j])
        for j, (i, to) in enumerate(
            zip([0, 1, 2, 2, 2, 3], [place.to_core, place.to_y] + place.to_z[1:] + [place.to_x])
        )
    ]

    early_copies = [
        corew[1], core0[1], *segw.y[0], *segw.y[1], *segw.z[0], *seg0.y[0], *seg0.z[0],
        out.x[3], out.core[3], *layer.x, *layer.core, *layer.far, seg1.x, seg2.x,
    ]
    for seg in (seg1, seg2):
        early_copies += [*seg.y[1], *seg.z[0], *seg.z[1]]

    def sent(copies):
        for copy in copies:
            copy.wait_send()

    def when(point):
        return pl.when(t == point)

    @when(0)
    def _():
        start(fetch_layer, operands(1), fetch_work, fetch_fold, fetch_gbt, operands(0))
        start(fetch, fetch_a1t)
        place.greet()
        fetch_layer.wait()
        for i in range(4):
            layer.send(i)
        fetch_work.wait()
        start(seg1.y[1], seg2.y[1])
        fetch_fold.wait()
        start(seg1.z[0][:2], seg2.z[0][:2])
        bqv_ref[...] = jnp.zeros_like(bqv_ref)
        sums_ref[0] = early_ref[...]
        da1_ref[...] = jnp.zeros_like(da1_ref)
        fetch_gbt.wait()

    def add_core():
        recv(corew[1])

        @pl.loop(0, Z_DEV)
        def _(z):
            workw_ref[1, z] = (
                workw_ref[1, z].astype(F32) + landw_ref[1, z].astype(F32)
            ).astype(BF16)

        start(segw.y[1])

    def wait(copies):
        for copy in copies:
            copy.wait()

    @when(0)
    def _():
        wait(operands(1))

    @when(4)
    def _():
        start(operands(3))
        wait(operands(0))

    @when(8)
    def _():
        start(operands(2))
        wait(operands(3))

    @when(9)
    def _():
        wait(operands(2))

    plan = [
        (2, 1, lambda: (seg1.fold_y(1, 0), seg1.fold_z(0))),
        (3, 1, lambda: layer.pass_on(0)),
        (4, 0, lambda: (seg1.fold_y(1, 1), seg2.fold_z(0))),
        (4, 1, lambda: layer.pass_on(1)),
        (5, 1, lambda: (seg1.fold_z(1), seg2.fold_y(1, 0))),
        (8, 0, lambda: (seg2.fold_y(1, 1), layer.pass_on(2))),
        (8, 1, lambda: (seg1.send_x(), segw.fold_y(0, 0), segw.fold_y(0, 1))),
        (9, 0, add_core),
        (9, 1, lambda: (seg2.fold_z(1), seg0.fold_y(0, 0), layer.pass_on(3))),
        (10, 1, lambda: segw.fold_z(0)),
        (11, 1, lambda: (seg2.send_x(), seg0.fold_y(0, 1))),
        (12, 1, lambda: (segw.fold_y(1, 0), segw.fold_y(1, 1))),
        (13, 1, lambda: (seg0.fold_z(0), out.pass_on(3))),
        (14, 1, lambda: segw.fold_z(1)),
    ]

    def serve(point):
        for at, where, act in plan:
            if where == point:
                pl.when(t == at)(lambda act=act: (act(), None)[1])

    @pl.when((t == 0) | (t == 4) | (t == 8) | (t == 9))
    def _():
        pick = (
            lax.broadcasted_iota(jnp.int32, (8, width), 1) // HEAD_DIM
            == lax.broadcasted_iota(jnp.int32, (8, width), 0)
        ).astype(BF16)

        @pl.loop(0, n // step)
        def _(i):
            rows = pl.ds(pl.multiple_of(i * step, step), step)
            columns = scale_ref[now, :, rows].T
            lane = lax.broadcasted_iota(jnp.int32, (step, width), 1)
            scale = columns[:, heads - 1 : heads]
            for h in reversed(range(heads - 1)):
                scale = jnp.where(lane < (h + 1) * HEAD_DIM, columns[:, h : h + 1], scale)
            do = (dot_nn(gb_ref[rows, :], gw_ref[now]) * scale).astype(BF16)
            do_ref[now, rows, :] = do
            product = do.astype(F32) * o_ref[now, rows, :].astype(F32)
            high = product.astype(BF16)
            low = (product - high.astype(F32)).astype(BF16)
            delta_ref[now, :, rows] = dot_nt(pick, high) + dot_nt(pick, low)

        dkv_ref[now] = jnp.zeros(dkv_ref.shape[1:], F32)
        value = dot_nn(gbt_ref[...], o_ref[now]).reshape(Z_DEV, Y_DEV, depth, width)
        for s in range(2):
            @when(8 * s)
            def _():
                if s:
                    corew[0].wait_send()
                stagew_ref[...] = value.astype(BF16)
                start(corew[s])

        @when(4)
        def _():
            recv(corew[0])
            workw_ref[0] = (value + landw_ref[0].astype(F32)).astype(BF16)
            start(segw.y[0])

        @when(9)
        def _():
            workw_ref[1] = value.astype(BF16)

    serve(0)

    for ii in reversed(range(4)):
        @pl.when(i == ii)
        def _():
            first, last = ii * step, (ii + 1) * step
            lane = lax.broadcasted_iota(jnp.int32, (1, width), 1)

            @pl.loop(0, heads)
            def _(h):
                here = (lane >= h * HEAD_DIM) & (lane < (h + 1) * HEAD_DIM)
                head = pl.ds(pl.multiple_of(h * HEAD_DIM, HEAD_DIM), HEAD_DIM)
                do = do_ref[now, first:last, :]
                q = q_ref[now, first:last, :]
                zero = jnp.zeros((), BF16)
                p = p_ref[0, h, :last, :]
                dp = dot_nt(v_ref[now, :last, :], jnp.where(here, do, zero))
                ds = p * (dp - delta_ref[now, pl.ds(h, 1), first:last]).astype(BF16)
                dqt_ref[head, :] = dot_nn(kt_ref[now, head, :last], ds)
                dkv_ref[now, 0, :last, :] += dot_nn(ds, jnp.where(here, q, zero))
                dkv_ref[now, 1, :last, :] += dot_nn(p, jnp.where(here, do, zero))

            dk = dkv_ref[now, 0, first:last, :].astype(BF16)
            dv = dkv_ref[now, 1, first:last, :].astype(BF16)
            dq = (dqt_ref[...] * HEAD_DIM ** -0.5).astype(BF16).T
            dqkv_ref[now, first:last, :width] = dq
            dqkv_ref[now, first:last, width : 2 * width] = dk
            dqkv_ref[now, first:last, 2 * width :] = dv
            bqv_ref[mine, 0:1, :] += jnp.sum(dq.astype(F32), 0, keepdims=True)
            bqv_ref[mine, 1:2, :] += jnp.sum(dv.astype(F32), 0, keepdims=True)
            da1_ref[first:last, :] += dot_nt(dqkv_ref[now, first:last, :], gq_ref[now])

    serve(1)

    @pl.when((t == 3) | (t == 7) | (t > 13))
    def _():
        @when(3)
        def _():
            fetch.wait()
            fetch_a1t.wait()

        value = dot_nn(a1t_ref[...], dqkv_ref[now]).reshape(Z_DEV, Y_DEV, depth, 3 * width)
        for s in range(2):
            @when(3 + 11 * s)
            def _():
                if s:
                    core0[0].wait_send()
                stage0_ref[...] = value.astype(BF16)
                start(core0[s])

            @when(7 + 8 * s)
            def _():
                recv(core0[s])
                work0_ref[s] = (value + land0_ref[s].astype(F32)).astype(BF16)
                if s:
                    tail.begin()
                else:
                    start(seg0.y[s])

    @pl.when((t > 8) & (t % 2 == 1))
    def _():
        rows = pl.ds(pl.multiple_of(i * step, step), step)
        xhat, r = norm_parts(own_ref[rows, :].astype(F32))
        da1 = da1_ref[rows, :]
        sums_ref[0, 0:1, :] += jnp.sum(da1 * xhat, 0, keepdims=True)
        sums_ref[0, 2:3, :] += jnp.sum(da1, 0, keepdims=True)
        dg = da1 * rows_ref[0:1, :]
        dv = r * (
            dg
            - jnp.mean(dg, -1, keepdims=True)
            - xhat * jnp.mean(dg * xhat, -1, keepdims=True)
        )
        own_ref[rows, :] = (dh1_ref[...] + dv).astype(BF16)
        for ii in range(4):
            @pl.when(i == ii)
            def _():
                out.send(ii)

    @when(15)
    def _():
        for s in range(4):
            sums_ref[0, 3:5, s * width : (s + 1) * width] = bqv_ref[s, 0:2, :]
        start(sum_core)
        segw.send_x()
        part1_ref[...] = seg1.total()
        part2_ref[...] = seg2.total()
        sent(early_copies)
        tail.fold_high()
        recv(sum_core)
        sums_ref[1] = sums_ref[0] + sumland_ref[0]
        start(sum_y)
        tail.fold_y()
        tail.cross_high()
        tail.fold_z()
        recv(sum_y)
        sums_ref[2] = sums_ref[1] + sumland_ref[1]
        start(sum_z)
        out.pass_on(2)
        tail.finish()
        start(seg0.x)
        recv(sum_z)
        sums_ref[3] = (sums_ref[2] + sumland_ref[2]) + (sumland_ref[3] + sumland_ref[4])
        start(sum_x)
        out.pass_on(1)
        partw_ref[...] = segw.total()
        layer.finish()
        out.pass_on(0)
        recv(sum_x)
        total_ref[...] = sums_ref[3] + sumland_ref[5]
        part0_ref[...] = seg0.total()
        out.finish()
        links.sent(corew[0], core0[0], *early_copies)


def group_and_block(t):
    early = t < 8
    return (
        jnp.where(early, 1 - t // 4, 3 - t % 2),
        3 - jnp.where(early, t % 4, jnp.maximum(t - 8, 0) // 2),
    )


def run_fused_backward(
    tokens, gq, gw, rows, dh1, gb, gbt, q, v, kt, p, scale, o, a1t, layer, fold, work, early
):
    groups, n, _ = tokens.shape
    width = gw.shape[-1]
    heads = width // HEAD_DIM
    hidden = fold.shape[-1]
    depth = D // (Z_DEV * Y_DEV)
    step = n // 4

    p_spec = pl.BlockSpec(
        (1, heads, n, step),
        lambda t: (group_and_block(t)[0], 0, 0, group_and_block(t)[1]),
    )

    copies = 12 + 12 + 4 + 15 + 2 * 11 + 8 + 11 + 6

    def landing(lanes, slots=1):
        return [
            pltpu.VMEM((slots, Z_DEV, depth, lanes), BF16),
            pltpu.VMEM((2, 3, depth, lanes), BF16), pltpu.VMEM((2, 2, depth, lanes), BF16),
            pltpu.VMEM((depth, lanes), BF16), pltpu.VMEM((depth, lanes), BF16),
        ]

    def working(lanes):
        block = (Z_DEV, Y_DEV, depth, lanes)
        return [pltpu.VMEM(block, BF16)] + [pltpu.VMEM((2,) + block, BF16)] * 2

    return pl.pallas_call(
        fused_backward,
        grid=(4 * groups,),
        in_specs=[
            ANY_WHOLE, ANY_WHOLE, ANY_WHOLE, VMEM_WHOLE,
            pl.BlockSpec((step, D), lambda t: (group_and_block(jnp.maximum(t, 8))[1], 0)),
            VMEM_WHOLE, ANY_WHOLE, ANY_WHOLE, ANY_WHOLE, ANY_WHOLE, p_spec,
            ANY_WHOLE, ANY_WHOLE, ANY_WHOLE, ANY_WHOLE, ANY_WHOLE, ANY_WHOLE, VMEM_WHOLE,
        ],
        out_specs=[ANY_WHOLE] * 2 + [VMEM_WHOLE] * 5,
        out_shape=[
            shaped(BF16, groups, n, D), shaped(BF16, groups, n, D),
            shaped(F32, depth, 3 * width),
            shaped(F32, depth, width), shaped(F32, depth, hidden),
            shaped(F32, depth, hidden), shaped(F32, 16, D),
        ],
        scratch_shapes=[
            pltpu.VMEM((2, D, 3 * width), BF16), pltpu.VMEM((2, D, width), BF16),
            pltpu.VMEM((2, n, width), BF16), pltpu.VMEM((2, n, width), BF16),
            pltpu.VMEM((2, width, n), BF16), pltpu.VMEM((2, 8, n), F32),
            pltpu.VMEM((2, n, width), BF16),
            pltpu.VMEM((D, n), BF16), pltpu.VMEM((D, n), BF16), pltpu.VMEM((n, D), BF16),
            pltpu.VMEM((2, Z_DEV, depth, hidden), BF16),
            pltpu.VMEM((2, Z_DEV, Y_DEV, depth, hidden), BF16),
            pltpu.VMEM((2, n, width), BF16),
            pltpu.VMEM((2, 8, n), F32), pltpu.VMEM((width, step), F32),
            pltpu.VMEM((2, 2, n, width), F32),
            pltpu.VMEM((2, n, 3 * width), BF16), pltpu.VMEM((n, D), F32),
            pltpu.VMEM((n, D), BF16), pltpu.VMEM((n, D), BF16), pltpu.VMEM((n, D), BF16),
            pltpu.VMEM((groups, 8, width), F32),
        ]
        + [pltpu.VMEM((2, Z_DEV, depth, hidden), BF16)] + landing(hidden) + landing(hidden)
        + working(width) + landing(width, 2)
        + working(3 * width) + landing(3 * width)
        + [
            pltpu.VMEM((4, 16, D), F32), pltpu.VMEM((6, 16, D), F32),
            pltpu.SemaphoreType.DMA((copies,)), pltpu.SemaphoreType.DMA((copies,)),
            pltpu.SemaphoreType.DMA((6,)), pltpu.SemaphoreType.DMA((2, 2, 4)),
            pltpu.SemaphoreType.DMA((2, 7)),
            pltpu.VMEM((Z_DEV, depth // 2, 3 * width), BF16),
            pltpu.VMEM((3, depth // 2, 3 * width), BF16),
            pltpu.VMEM((2, depth // 2, 3 * width), BF16),
            pltpu.VMEM((3, Y_DEV, depth // 2, 3 * width), BF16),
            pltpu.VMEM((2, Y_DEV, depth // 2, 3 * width), BF16),
            pltpu.VMEM((Y_DEV, depth // 2, 3 * width), BF16),
            pltpu.VMEM((depth // 2, 3 * width), BF16),
        ],
        compiler_params=pltpu.CompilerParams(
            vmem_limit_bytes=VMEM_LIMIT, collective_id=2, has_side_effects=True
        ),
        name="fused_backward",
    )(tokens, gq, gw, rows, dh1, gb, gbt, q, v, kt, p, scale, o, a1t, layer, fold, work, early)


def place_gradients(
    tie_ref, sums_ref, part0_ref, partw_ref, part1_ref, part2_ref, near_out_ref,
    near_grad_ref, far_out_ref, far_grad_ref, gains_ref, bias_ref, in_ref, out_ref, expand_ref,
    project_ref,
):
    far_out_ref[...] = near_out_ref[...]
    far_grad_ref[...] = near_grad_ref[...]
    own = gains_ref.shape[-1]
    width = partw_ref.shape[-1]

    @pl.when(pl.program_id(0) == 0)
    def _():
        first = (lax.axis_index("dp") * 4 + lax.axis_index("tensor")) * own
        feature = lax.broadcasted_iota(jnp.int32, (D, 128), 0)
        lane = lax.broadcasted_iota(jnp.int32, (D, 128), 1)
        chosen = ((feature == first + lane) & (lane < own)).astype(F32)
        sums = lax.dot_general(
            sums_ref[...], chosen, (((1,), (0,)), ((), ())),
            precision=lax.Precision.HIGHEST, preferred_element_type=F32,
        )[:, :own]
        s0, s1, s2, s3 = tie_ref[0], tie_ref[1], tie_ref[2], tie_ref[3]
        w_out = partw_ref[...].T

        def at(source, wanted, value):
            return jnp.where(source == wanted, value, jnp.zeros_like(value))

        row = lax.broadcasted_iota(jnp.int32, (NSRC, own), 0)
        for i, wanted in enumerate([s0, s0, s0, s1, s2, s3, s2, s2, s2, s2]):
            bias_ref[i] = jnp.where(row == wanted, sums[2 + i : 3 + i], 0.0)
        for s in range(NSRC):
            gains_ref[s, 0:1] = at(s, s0, sums[0:1])
            gains_ref[s, 1:2] = at(s, s2, sums[1:2])
            for j in range(3):
                in_ref[s, j] = at(s, s0, part0_ref[:, j * width : (j + 1) * width])
            out_ref[s] = at(s, s1, w_out)
            expand_ref[s] = at(s, s2, part1_ref[...])
            project_ref[s] = at(s, s3, part2_ref[...])


def run_place_gradients(tie, sums, part0, partw, part1, part2, out, grad, like):
    slots, n, _ = grad.shape
    gains, biases, w_in, w_out, w_expand, w_project = [item.shape for item in like]
    shapes = [
        gains, (biases[1], biases[0], biases[2]), w_in, w_out, w_expand,
        (w_project[0], w_project[2], w_project[1]),
    ]
    out, grad, gains, biases, w_in, w_out, w_expand, w_project = pl.pallas_call(
        place_gradients,
        grid=(slots,),
        in_specs=[SMEM_WHOLE] + [VMEM_WHOLE] * 5
        + [group(n, D), group(n, D)],
        out_specs=[group(n, D), group(n, D)] + [VMEM_WHOLE] * 6,
        out_shape=[shaped(BF16, slots, n, D)] * 2 + [shaped(F32, *item) for item in shapes],
        compiler_params=pltpu.CompilerParams(vmem_limit_bytes=VMEM_LIMIT),
        name="place_gradients",
    )(tie, sums, part0, partw, part1, part2, out, grad)
    biases = biases.transpose(1, 0, 2)
    return out, grad, gains, biases, w_in, w_out, w_expand, w_project.transpose(0, 2, 1)


def plain_step(
    tokens, lengths, tie_map, norm_gains, bias_rows, attention_in, attention_out,
    expand_weight, project_weight, cotangent,
):
    slot_rows = tokens.shape[0] // lengths.shape[0]
    me = lax.axis_index("tensor")
    in_local = lax.dynamic_index_in_dim(attention_in, tie_map[0], 0, keepdims=False)
    out_local = lax.dynamic_index_in_dim(attention_out, tie_map[1], 0, keepdims=False)
    expand_local = lax.dynamic_index_in_dim(expand_weight, tie_map[2], 0, keepdims=False)
    project_local = lax.dynamic_index_in_dim(project_weight, tie_map[3], 0, keepdims=False)
    local0 = jnp.concatenate([in_local, out_local.T[None]], 0)
    row_kinds = jnp.array([0, 0, 0, 1, 2, 3] + [2] * (FF // D), dtype=jnp.int32)
    gain_kinds = jnp.array([0, 2], dtype=jnp.int32)
    gain_pick = norm_gains[tie_map[gain_kinds], jnp.arange(2)]
    bias_pick = bias_rows[tie_map[row_kinds], jnp.arange(row_kinds.shape[0])]
    vectors = jnp.concatenate([gain_pick, bias_pick], 0)
    x = lax.dynamic_slice_in_dim(tokens, me * slot_rows, slot_rows, 0)
    cot = lax.dynamic_slice_in_dim(cotangent, me * slot_rows, slot_rows, 0)
    length = lax.dynamic_slice_in_dim(lengths, me, 1, 0)
    rows = lax.all_gather(vectors, ("dp", "tensor"), axis=1, tiled=True).astype(F32)
    rows = jnp.concatenate([rows, jnp.zeros((4, D), F32)], 0)

    def gathered(piece, axis):
        piece = lax.all_gather(piece, "dp", axis=axis, tiled=True)
        return lax.all_gather(piece, "tensor", axis=0)

    g0 = gathered(local0, 1)
    g1 = gathered(expand_local, 0)
    g2 = gathered(project_local.T, 0)
    groups, width = g0.shape[0], g0.shape[-1]
    bqv = rows[3:5].reshape(2, groups, width).transpose(1, 0, 2)
    q, v, kt, p, o, a1t, h1, a2, a2t = run_attention_forward(length, x, g0, rows, bqv)
    out, d1, d2, dh1, gb, gbt, sums = run_feed_forward(length, cot, a2, a2t, h1, g1, g2, rows)
    d0, xg, sums_in, sums_qv = run_attention_backward(
        x, g0, rows, dh1, gb, gbt, q, v, kt, p, o, a1t
    )
    layer_out = lax.all_gather(out, "tensor", axis=0, tiled=True)
    tokens_grad = lax.all_gather(xg, "tensor", axis=0, tiled=True)

    def scattered(piece, axis):
        piece = lax.psum_scatter(piece, "tensor", scatter_dimension=0)
        return lax.psum_scatter(piece, "dp", scatter_dimension=axis, tiled=True).astype(F32)

    part0 = scattered(d0, 1)
    part1 = scattered(d1, 0)
    part2 = scattered(d2, 0)
    qv = sums_qv[:, :2].transpose(1, 0, 2).reshape(2, D)
    sums = jnp.concatenate(
        [sums_in[0:1], sums[1:2], sums_in[1:2], qv, sums[5:12]], 0
    )
    sums = lax.psum_scatter(sums, ("dp", "tensor"), scatter_dimension=1, tiled=True)
    return layer_out, tokens_grad, *placed(tie_map, sums, part0, part1, part2)


def fused_step(
    tokens, lengths, tie_map, norm_gains, bias_rows, attention_in, attention_out,
    expand_weight, project_weight, cotangent,
):
    slots = lengths.shape[0]
    tokens = tokens.reshape(slots, -1, D)
    cotangent = cotangent.reshape(slots, -1, D)
    gq, gw, g1, g2, rows, q, v, kt, p, scale, o, a1t, h1, a2, a2t = run_fused_forward(
        tie_map, lengths, tokens, norm_gains, bias_rows, attention_in, attention_out,
        expand_weight, project_weight,
    )
    layer, fold, work, dh1, gb, gbt, early = run_fused_feed_forward(
        lengths, cotangent, a2, a2t, h1, g1, g2, rows
    )
    grad, out, part0, partw, part1, part2, sums = run_fused_backward(
        tokens, gq, gw, rows, dh1, gb, gbt, q, v, kt, p, scale, o, a1t, layer, fold,
        work, early,
    )
    out, grad, *placed_grads = run_place_gradients(
        tie_map, sums, part0, partw, part1, part2, out, grad,
        (norm_gains, bias_rows, attention_in, attention_out, expand_weight, project_weight),
    )
    return out.reshape(-1, D), grad.reshape(-1, D), *placed_grads


def placed(tie_map, sums, part0, part1, part2):
    source = jnp.arange(NSRC, dtype=jnp.int32)

    def place(piece, which):
        pick = (source == tie_map[which]).reshape((NSRC,) + (1,) * piece.ndim)
        return jnp.where(pick, piece[None], 0.0)

    def place_rows(piece, kinds):
        pick = source[:, None] == tie_map[jnp.array(kinds, dtype=jnp.int32)][None, :]
        return jnp.where(pick[:, :, None], piece[None], 0.0)

    return (
        place_rows(sums[:2], [0, 2]),
        place_rows(sums[2:], [0, 0, 0, 1, 2, 3] + [2] * (FF // D)),
        place(part0[:3], 0),
        place(part0[3].T, 1),
        place(part1, 2),
        place(part2.T, 3),
    )


def solution(mesh):
    fused = mesh.shape["dp"] == Z_DEV * Y_DEV and mesh.shape["tensor"] == X_DEV * C_DEV
    return jax.shard_map(
        fused_step if fused else plain_step,
        mesh=mesh,
        in_specs=(
            P("dp", None),
            P("dp"),
            P(),
            P(None, None, ("dp", "tensor")),
            P(None, None, ("dp", "tensor")),
            P(None, None, "dp", "tensor"),
            P(None, "tensor", "dp"),
            P(None, "dp", "tensor"),
            P(None, "tensor", "dp"),
            P("dp", None),
        ),
        out_specs=(
            P("dp", None),
            P("dp", None),
            P(None, None, ("dp", "tensor")),
            P(None, None, ("dp", "tensor")),
            P(None, None, "dp", "tensor"),
            P(None, "tensor", "dp"),
            P(None, "dp", "tensor"),
            P(None, "tensor", "dp"),
        ),
        check_vma=False,
    )
```

```python
import jax
import jax.numpy as jnp
from jax import lax
from jax.experimental import pallas as pl
from jax.experimental.pallas import tpu as pltpu
from jax.sharding import PartitionSpec as P

D = 768
HEAD_DIM = 64
FF = 3072
NSRC = 4
EPS = 1e-05
MASKED = -1e30
F32 = jnp.float32
BF16 = jnp.bfloat16
VMEM_LIMIT = 60 * 1024 * 1024


def dot_nn(a, b):
    return lax.dot_general(a, b, (((1,), (0,)), ((), ())), preferred_element_type=F32)


def dot_nt(a, b):
    return lax.dot_general(a, b, (((1,), (1,)), ((), ())), preferred_element_type=F32)


def norm_parts(v):
    center = jnp.mean(v, -1, keepdims=True)
    centered = v - center
    r = lax.rsqrt(jnp.mean(centered * centered, -1, keepdims=True) + EPS)
    return centered * r, r


def head_mask(shape, h):
    lane = lax.broadcasted_iota(jnp.int32, shape, 1)
    return (lane >= h * HEAD_DIM) & (lane < (h + 1) * HEAD_DIM)


def blocks(total, size):
    return [slice(i * size, (i + 1) * size) for i in range(total // size)]


def attention_forward(
    len_ref, x_ref, g_ref, rows_ref, bqv_ref,
    q_ref, v_ref, kt_ref, p_ref, o_ref, a1t_ref, h1_ref, a2_ref, a2t_ref,
    a1_ref, k_ref, vt_ref, ot_ref, attn_ref,
):
    t = pl.program_id(0)
    n = x_ref.shape[0]
    width = g_ref.shape[-1]
    heads = width // HEAD_DIM
    step = 256
    length = len_ref[0]

    @pl.when(t == 0)
    def _():
        @pl.loop(0, n // step)
        def _(b):
            rows = pl.ds(pl.multiple_of(b * step, step), step)
            xhat, _ = norm_parts(x_ref[rows, :].astype(F32))
            a1 = xhat * rows_ref[0:1, :] + rows_ref[2:3, :]
            a1_ref[rows, :] = a1.astype(BF16)
            a1t_ref[:, rows] = a1.astype(BF16).T
            attn_ref[rows, :] = x_ref[rows, :].astype(F32) + rows_ref[5:6, :]

    @pl.loop(0, n // step)
    def _(b):
        rows = pl.ds(pl.multiple_of(b * step, step), step)
        a1 = a1_ref[rows, :]
        q = (dot_nn(a1, g_ref[0, 0]) + bqv_ref[0, 0:1, :]).astype(BF16)
        q_ref[0, rows, :] = q * jnp.asarray(HEAD_DIM ** -0.5, BF16)
        k = dot_nn(a1, g_ref[0, 1]).astype(BF16)
        k_ref[rows, :] = k
        kt_ref[0, :, rows] = k.T
        v = (dot_nn(a1, g_ref[0, 2]) + bqv_ref[0, 1:2, :]).astype(BF16)
        v_ref[0, rows, :] = v
        vt_ref[:, rows] = v.T

    for h in range(heads):
        k = k_ref[...]
        k = jnp.where(head_mask(k.shape, h), k, jnp.zeros_like(k))
        for b in range(n // step):
            first, last = b * step, (b + 1) * step
            q = q_ref[0, first:last, :]
            key = lax.broadcasted_iota(jnp.int32, (last, step), 0)
            query = lax.broadcasted_iota(jnp.int32, (step, step), 1) + first
            s = dot_nt(k[:last], q)
            near = jnp.where(
                (key[first:] <= query) & (key[first:] < length), s[first:], MASKED
            )
            if b:
                far = jnp.where(key[:first] < length, s[:first], MASKED)
                top = jnp.maximum(
                    jnp.max(far, 0, keepdims=True), jnp.max(near, 0, keepdims=True)
                )
                e_far = jnp.exp(far - top)
                e_near = jnp.exp(near - top)
                total = jnp.sum(e_far, 0, keepdims=True) + jnp.sum(e_near, 0, keepdims=True)
                scale = 1.0 / total
                p_ref[0, h, :first, first:last] = (e_far * scale).astype(BF16)
            else:
                top = jnp.max(near, 0, keepdims=True)
                e_near = jnp.exp(near - top)
                scale = 1.0 / jnp.sum(e_near, 0, keepdims=True)
            p_ref[0, h, first:last, first:last] = (e_near * scale).astype(BF16)
            ot_ref[h * HEAD_DIM : (h + 1) * HEAD_DIM, first:last] = dot_nn(
                vt_ref[h * HEAD_DIM : (h + 1) * HEAD_DIM, :last],
                p_ref[0, h, :last, first:last],
            ).astype(BF16)

    @pl.loop(0, n // step)
    def _(b):
        rows = pl.ds(pl.multiple_of(b * step, step), step)
        o = ot_ref[:, rows].T
        o_ref[0, rows, :] = o
        attn_ref[rows, :] += dot_nt(o, g_ref[0, 3])

    @pl.when(t == pl.num_programs(0) - 1)
    def _():
        @pl.loop(0, n // step)
        def _(b):
            rows = pl.ds(pl.multiple_of(b * step, step), step)
            h1 = attn_ref[rows, :]
            h1_ref[rows, :] = h1
            xhat, _ = norm_parts(h1)
            a2 = (xhat * rows_ref[1:2, :] + rows_ref[6:7, :]).astype(BF16)
            a2_ref[rows, :] = a2
            a2t_ref[:, rows] = a2.T


SQRT_2_PI = 0.7978845608028654


def feed_forward_both(
    len_ref, c_ref, a2_ref, a2t_ref, h1_ref, w1_ref, w2_ref, rows_ref,
    out_ref, d1_ref, d2_ref, dh1_ref, gb_ref, gbt_ref, sums_ref,
    gf_ref, gft_ref, feed_ref, da2_ref, h_ref, df_ref,
):
    t = pl.program_id(0)
    n = c_ref.shape[0]
    step = 256
    length = len_ref[0]

    @pl.when(t == 0)
    def _():
        sums_ref[...] = jnp.zeros_like(sums_ref)

        @pl.loop(0, n // step)
        def _(b):
            rows = pl.ds(pl.multiple_of(b * step, step), step)
            place = b * step + lax.broadcasted_iota(jnp.int32, (step, 1), 0)
            live = (place < length).astype(F32)
            g = (c_ref[rows, :].astype(F32) * live).astype(BF16)
            gf_ref[rows, :] = g
            gft_ref[:, rows] = g.T
            sums_ref[7:8, :] += jnp.sum(g.astype(F32), 0, keepdims=True)

    bias = rows_ref[pl.ds(8 + t, 1), :]

    @pl.loop(0, n // step)
    def _(b):
        rows = pl.ds(pl.multiple_of(b * step, step), step)
        f = dot_nn(a2_ref[rows, :], w1_ref[0]) + bias
        dh = dot_nn(gf_ref[rows, :], w2_ref[0])
        f2 = f * f
        th = jnp.tanh(f * (SQRT_2_PI + (SQRT_2_PI * 0.044715) * f2))
        half = 0.5 + 0.5 * th
        h = (f * half).astype(BF16)
        slope = half + f * (0.5 - 0.5 * th * th) * (
            SQRT_2_PI + (3 * SQRT_2_PI * 0.044715) * f2
        )
        df = (dh * slope).astype(BF16)
        h_ref[rows, :] = h
        df_ref[rows, :] = df
        sums_ref[pl.ds(8 + t, 1), :] += jnp.sum(df.astype(F32), 0, keepdims=True)
        feed = dot_nt(h, w2_ref[0])
        da2 = dot_nt(df, w1_ref[0])

        @pl.when(t == 0)
        def _():
            feed_ref[rows, :] = feed
            da2_ref[rows, :] = da2

        @pl.when(t > 0)
        def _():
            feed_ref[rows, :] += feed
            da2_ref[rows, :] += da2

    @pl.loop(0, D // step)
    def _(b):
        rows = pl.ds(pl.multiple_of(b * step, step), step)
        d1_ref[0, rows, :] = dot_nn(a2t_ref[rows, :], df_ref[...]).astype(BF16)
        d2_ref[0, rows, :] = dot_nn(gft_ref[rows, :], h_ref[...]).astype(BF16)

    @pl.when(t == pl.num_programs(0) - 1)
    def _():
        @pl.loop(0, n // step)
        def _(b):
            rows = pl.ds(pl.multiple_of(b * step, step), step)
            place = b * step + lax.broadcasted_iota(jnp.int32, (step, 1), 0)
            live = (place < length).astype(F32)
            h1 = h1_ref[rows, :]
            out_ref[rows, :] = (live * (h1 + (feed_ref[rows, :] + rows_ref[7:8, :]))).astype(BF16)
            xhat, r = norm_parts(h1)
            da2 = da2_ref[rows, :]
            sums_ref[1:2, :] += jnp.sum(da2 * xhat, 0, keepdims=True)
            sums_ref[6:7, :] += jnp.sum(da2, 0, keepdims=True)
            dg = da2 * rows_ref[1:2, :]
            dv = r * (
                dg
                - jnp.mean(dg, -1, keepdims=True)
                - xhat * jnp.mean(dg * xhat, -1, keepdims=True)
            )
            dh1 = live * c_ref[rows, :].astype(F32) + dv
            dh1_ref[rows, :] = dh1
            gb = dh1.astype(BF16)
            gb_ref[rows, :] = gb
            gbt_ref[:, rows] = gb.T
            sums_ref[5:6, :] += jnp.sum(gb.astype(F32), 0, keepdims=True)


def attention_backward(
    x_ref, g_ref, rows_ref, dh1_ref, gb_ref, gbt_ref, q_ref, v_ref, kt_ref, p_ref,
    o_ref, a1t_ref,
    d0_ref, xg_ref, sums_ref, bqv_ref,
    do_ref, delta_ref, dqt_ref, dq_ref, dk_ref, dv_ref, da1_ref,
):
    t = pl.program_id(0)
    n = x_ref.shape[0]
    width = g_ref.shape[-1]
    heads = width // HEAD_DIM
    step = 256
    pick = (
        lax.broadcasted_iota(jnp.int32, (16, width), 1) // HEAD_DIM
        == lax.broadcasted_iota(jnp.int32, (16, width), 0)
    ).astype(BF16)

    @pl.loop(0, n // step)
    def _(b):
        rows = pl.ds(pl.multiple_of(b * step, step), step)
        do = dot_nn(gb_ref[rows, :], g_ref[0, 3]).astype(BF16)
        do_ref[rows, :] = do
        prod = do.astype(F32) * o_ref[0, rows, :].astype(F32)
        high = prod.astype(BF16)
        low = (prod - high.astype(F32)).astype(BF16)
        delta_ref[:, rows] = dot_nt(pick, high) + dot_nt(pick, low)

    dqt_ref[...] = jnp.zeros_like(dqt_ref)
    for b in range(n // step):
        first, last = b * step, (b + 1) * step
        do = do_ref[first:, :]
        q = q_ref[0, first:, :]
        v = v_ref[0, first:last, :]
        dk, dv = None, None
        for h in range(heads):
            mine = head_mask((1, width), h)
            zero = jnp.zeros((), BF16)
            p = p_ref[0, h, first:last, first:]
            dp = dot_nt(jnp.where(mine, v, zero), do)
            ds = (p.astype(F32) * (dp - delta_ref[h : h + 1, first:])).astype(BF16)
            part = dot_nn(p, jnp.where(mine, do, zero))
            dv = part if dv is None else dv + part
            part = dot_nn(ds, jnp.where(mine, q, zero))
            dk = part if dk is None else dk + part
            head = slice(h * HEAD_DIM, (h + 1) * HEAD_DIM)
            dqt_ref[head, first:] += dot_nn(kt_ref[0, head, first:last], ds)
        dk_ref[first:last, :] = dk.astype(BF16)
        dv_ref[first:last, :] = dv.astype(BF16)

    @pl.when(t == 0)
    def _():
        da1_ref[...] = jnp.zeros_like(da1_ref)

    bqv_ref[...] = jnp.zeros_like(bqv_ref)

    @pl.loop(0, n // step)
    def _(b):
        rows = pl.ds(pl.multiple_of(b * step, step), step)
        dq = (dqt_ref[:, rows] * HEAD_DIM ** -0.5).astype(BF16).T
        dk = dk_ref[rows, :]
        dv = dv_ref[rows, :]
        dq_ref[rows, :] = dq
        bqv_ref[0, 0:1, :] += jnp.sum(dq.astype(F32), 0, keepdims=True)
        bqv_ref[0, 1:2, :] += jnp.sum(dv.astype(F32), 0, keepdims=True)
        da1_ref[rows, :] += (
            dot_nt(dq, g_ref[0, 0]) + dot_nt(dk, g_ref[0, 1]) + dot_nt(dv, g_ref[0, 2])
        )

    @pl.loop(0, D // step)
    def _(b):
        rows = pl.ds(pl.multiple_of(b * step, step), step)
        a1t = a1t_ref[rows, :]
        d0_ref[0, 0, rows, :] = dot_nn(a1t, dq_ref[...]).astype(BF16)
        d0_ref[0, 1, rows, :] = dot_nn(a1t, dk_ref[...]).astype(BF16)
        d0_ref[0, 2, rows, :] = dot_nn(a1t, dv_ref[...]).astype(BF16)
        d0_ref[0, 3, rows, :] = dot_nn(gbt_ref[rows, :], o_ref[0]).astype(BF16)

    @pl.when(t == pl.num_programs(0) - 1)
    def _():
        sums_ref[...] = jnp.zeros_like(sums_ref)

        @pl.loop(0, n // step)
        def _(b):
            rows = pl.ds(pl.multiple_of(b * step, step), step)
            xhat, r = norm_parts(x_ref[rows, :].astype(F32))
            da1 = da1_ref[rows, :]
            sums_ref[0:1, :] += jnp.sum(da1 * xhat, 0, keepdims=True)
            sums_ref[1:2, :] += jnp.sum(da1, 0, keepdims=True)
            dg = da1 * rows_ref[0:1, :]
            dv = r * (
                dg
                - jnp.mean(dg, -1, keepdims=True)
                - xhat * jnp.mean(dg * xhat, -1, keepdims=True)
            )
            xg_ref[rows, :] = (dh1_ref[rows, :] + dv).astype(BF16)


def whole(*shape):
    return pl.BlockSpec(shape, lambda t: (0,) * len(shape))


def group(*shape):
    return pl.BlockSpec((1,) + shape, lambda t: (t,) + (0,) * len(shape))


def shaped(dtype, *shape):
    return jax.ShapeDtypeStruct(shape, dtype)


SMEM_WHOLE = pl.BlockSpec(memory_space=pltpu.SMEM)


def run_attention_forward(length, x, g0, rows, bqv):
    n = x.shape[0]
    groups, _, _, width = g0.shape
    heads = width // HEAD_DIM
    return pl.pallas_call(
        attention_forward,
        grid=(groups,),
        in_specs=[SMEM_WHOLE, whole(n, D), group(4, D, width), whole(16, D), group(2, width)],
        out_specs=[
            group(n, width), group(n, width), group(width, n), group(heads, n, n),
            group(n, width), whole(D, n), whole(n, D), whole(n, D), whole(D, n),
        ],
        out_shape=[
            shaped(BF16, groups, n, width), shaped(BF16, groups, n, width),
            shaped(BF16, groups, width, n), shaped(BF16, groups, heads, n, n),
            shaped(BF16, groups, n, width), shaped(BF16, D, n), shaped(F32, n, D),
            shaped(BF16, n, D), shaped(BF16, D, n),
        ],
        scratch_shapes=[
            pltpu.VMEM((n, D), BF16), pltpu.VMEM((n, width), BF16),
            pltpu.VMEM((width, n), BF16), pltpu.VMEM((width, n), BF16),
            pltpu.VMEM((n, D), F32),
        ],
        compiler_params=pltpu.CompilerParams(vmem_limit_bytes=VMEM_LIMIT),
        name="attention_forward",
    )(length, x, g0, rows, bqv)


def run_feed_forward(length, cot, a2, a2t, h1, g1, g2, rows):
    n = cot.shape[0]
    groups, _, width = g1.shape
    return pl.pallas_call(
        feed_forward_both,
        grid=(groups,),
        in_specs=[
            SMEM_WHOLE, whole(n, D), whole(n, D), whole(D, n), whole(n, D),
            group(D, width), group(D, width), whole(16, D),
        ],
        out_specs=[
            whole(n, D), group(D, width), group(D, width), whole(n, D), whole(n, D),
            whole(D, n), whole(16, D),
        ],
        out_shape=[
            shaped(BF16, n, D), shaped(BF16, groups, D, width), shaped(BF16, groups, D, width),
            shaped(F32, n, D), shaped(BF16, n, D), shaped(BF16, D, n), shaped(F32, 16, D),
        ],
        scratch_shapes=[
            pltpu.VMEM((n, D), BF16), pltpu.VMEM((D, n), BF16), pltpu.VMEM((n, D), F32),
            pltpu.VMEM((n, D), F32), pltpu.VMEM((n, width), BF16), pltpu.VMEM((n, width), BF16),
        ],
        compiler_params=pltpu.CompilerParams(vmem_limit_bytes=VMEM_LIMIT),
        name="feed_forward_both",
    )(length, cot, a2, a2t, h1, g1, g2, rows)


def run_attention_backward(x, g0, rows, dh1, gb, gbt, q, v, kt, p, o, a1t):
    n = x.shape[0]
    groups, _, _, width = g0.shape
    heads = width // HEAD_DIM
    return pl.pallas_call(
        attention_backward,
        grid=(groups,),
        in_specs=[
            whole(n, D), group(4, D, width), whole(16, D), whole(n, D), whole(n, D),
            whole(D, n), group(n, width), group(n, width), group(width, n),
            group(heads, n, n), group(n, width), whole(D, n),
        ],
        out_specs=[group(4, D, width), whole(n, D), whole(8, D), group(8, width)],
        out_shape=[
            shaped(BF16, groups, 4, D, width), shaped(BF16, n, D), shaped(F32, 8, D),
            shaped(F32, groups, 8, width),
        ],
        scratch_shapes=[
            pltpu.VMEM((n, width), BF16), pltpu.VMEM((16, n), F32), pltpu.VMEM((width, n), F32),
            pltpu.VMEM((n, width), BF16), pltpu.VMEM((n, width), BF16),
            pltpu.VMEM((n, width), BF16), pltpu.VMEM((n, D), F32),
        ],
        compiler_params=pltpu.CompilerParams(vmem_limit_bytes=VMEM_LIMIT),
        name="attention_backward",
    )(x, g0, rows, dh1, gb, gbt, q, v, kt, p, o, a1t)


Z_DEV, Y_DEV, X_DEV, C_DEV = 4, 2, 2, 2


class Place:
    def __init__(self):
        dp, self.t = lax.axis_index("dp"), lax.axis_index("tensor")
        self.dp = dp
        self.z, self.y = dp // 2, dp % 2
        self.x, self.c = self.t // 2, self.t % 2
        self.other_y = 1 - self.y
        self.zs = [
            self.z,
            self.z + 1 - 2 * (self.z % 2),
            self.z + 2 - 4 * (self.z // 2),
            3 - self.z,
        ]
        self.ts = [
            self.t,
            self.t + 1 - 2 * (self.t % 2),
            self.t + 2 - 4 * (self.t // 2),
            3 - self.t,
        ]
        self.to_z = [dict(dp=z * 2 + self.y) for z in self.zs]
        self.to_y = dict(dp=self.z * 2 + self.other_y)
        self.to_x = dict(tensor=self.ts[2])
        self.same_t = self.to_z[1:] + [dict(dp=z * 2 + self.other_y) for z in self.zs]
        self.same_dp = [dict(tensor=t) for t in self.ts[1:]]
        self.to_core = dict(tensor=self.ts[1])

    def group(self, k):
        return lax.select(
            k == 0, self.ts[0],
            lax.select(k == 1, self.ts[1], lax.select(k == 2, self.ts[2], self.ts[3])),
        )

    def greet(self, others=None):
        barrier = pltpu.get_barrier_semaphore()
        others = others or self.to_z[1:] + [self.to_y, self.to_x, self.to_core]
        for device in others:
            pl.semaphore_signal(
                barrier, inc=1, device_id=device, device_id_type=pl.DeviceIdType.MESH
            )
        pl.semaphore_wait(barrier, len(others))


class Links:
    def __init__(self, send_sem, recv_sem):
        self.send_sem, self.recv_sem = send_sem, recv_sem
        self.copies = []

    def add(self, device, src, dst):
        number = len(self.copies)
        copy = pltpu.make_async_remote_copy(
            src_ref=src,
            dst_ref=dst,
            send_sem=self.send_sem.at[number],
            recv_sem=self.recv_sem.at[number],
            device_id=device,
            device_id_type=pl.DeviceIdType.MESH,
        )
        self.copies.append(copy)
        return copy

    def sent(self, *apart):
        for copy in self.copies:
            if all(copy is not other for other in apart):
                copy.wait_send()


def flat(copies):
    for item in copies:
        if isinstance(item, list):
            yield from flat(item)
        else:
            yield item


def start(*copies):
    for copy in flat(copies):
        copy.start()


def recv(*copies):
    for copy in flat(copies):
        copy.wait_recv()


class Gather:
    def __init__(self, links, place, own, full, order, single=True, last=True):
        every = slice(None)
        y, other = place.y, place.other_y

        def same(device, k, yy, to):
            return links.add(device, full(k, every, yy), full(to, every, yy))

        def along_z(k, yy, block):
            here, passed = full(k, place.z, yy), full(k, place.zs[2], yy)
            return [
                links.add(place.to_z[1], block, here),
                links.add(place.to_z[2], block, here),
                links.add(place.to_z[1], passed, passed),
            ]

        self.z = along_z(0, y, own)
        if order == X_Z_Y:
            self.first = [links.add(place.to_x, own, full(2, place.z, y))]
            self.far = along_z(2, y, full(2, place.z, y))
            blocks = [(0, y), (2, y), (0, other), (2, other)]
        else:
            blocks = [(0, y), (0, other), (2, y), (2, other)]
        if order == Y_Z_X:
            self.first = [links.add(place.to_y, own, full(0, place.z, y))]
            self.far = along_z(0, other, full(0, place.z, other))
        if order == Z_Y_X and single:
            self.first = [same(place.to_y, 0, y, 0)]
        if order == Z_Y_X and not single:
            self.first = [links.add(place.to_y, own, full(0, place.z, y))]
            for k in range(1, 4):
                block = full(0, place.zs[k], y)
                self.first.append(links.add(place.to_y, block, block))
        self.second = [
            same(place.to_y, k, yy, k) if order == X_Z_Y else same(place.to_x, k, yy, 2)
            for k, yy in blocks[: 2 if last else 1]
            if last or order == X_Z_Y
        ]
        if order == Y_Z_X and not last:
            part = pl.ds(0, Z_DEV // 2)
            self.second = [links.add(place.to_x, full(0, part, y), full(2, part, y))]
        if not last:
            blocks = [block for block in blocks if block[0] == 0]
        self.core = [same(place.to_core, k, yy, k + 1) for k, yy in blocks]


Z_Y_X, Y_Z_X, X_Z_Y = range(3)


def fused_forward(
    tie_ref, len_ref, tokens_ref, gains_ref, bias_ref, in_ref, out_ref, expand_ref,
    project_ref,
    gq_ref, gw_ref, flat1_ref, flat2_ref, rows_ref,
    q_ref, v_ref, kt_ref, p_ref, scale_ref, o_ref, a1t_out, h1_out, a2_out, a2t_out,
    own0_ref, ownw_ref, own1_ref, own2_ref, square_ref, vec_ref,
    all0_ref, allw_ref, w1_ref, w2_ref, vecs_ref, bqv_ref, x_ref, a1_ref, k_ref, qa_ref, vt_ref, ot_ref, a1t_ref, h1_ref, a2_ref, a2t_ref,
    send_sem, recv_sem, local_sem, flush_sem, row_sem,
):
    t = pl.program_id(0)
    n, _ = x_ref.shape
    width = allw_ref.shape[-1]
    heads = width // HEAD_DIM
    step = 256
    place = Place()
    length = len_ref[place.t]
    links = Links(send_sem, recv_sem)
    z, y, x, c = place.z, place.y, place.x, place.c
    mine_there = vecs_ref.at[z, y, x, c]
    column = vecs_ref.at[:, :, x, c]
    vec_one = [links.add(device, vec_ref, mine_there) for device in place.same_t]
    vec_two = [links.add(device, column, column) for device in place.same_dp]
    seg0 = Gather(
        links, place, own0_ref, lambda k, z, y: all0_ref.at[k, z, y], Z_Y_X, single=False
    )
    segw = Gather(links, place, ownw_ref, lambda k, z, y: allw_ref.at[k, z, y], Z_Y_X)
    seg1 = Gather(
        links, place, own1_ref, lambda k, z, y: w1_ref.at[k, z, y], Y_Z_X, last=False
    )
    seg2 = Gather(
        links, place, own2_ref, lambda k, z, y: w2_ref.at[k, z, y], X_Z_Y, last=False
    )
    flush = [
        [
            pltpu.make_async_copy(ref.at[k], flat.at[k], flush_sem.at[i, k])
            for k in range(3)
        ]
        for i, (ref, flat) in enumerate([(w1_ref, flat1_ref), (w2_ref, flat2_ref)])
    ]
    put_a1t = pltpu.make_async_copy(a1t_ref, a1t_out, local_sem.at[0])
    put_a2t = pltpu.make_async_copy(a2t_ref, a2t_out, local_sem.at[1])
    puts = []
    for i in range(n // step):
        rows = pl.ds(i * step, step)
        puts.append([
            pltpu.make_async_copy(h1_ref.at[rows], h1_out.at[rows], row_sem.at[0, i]),
            pltpu.make_async_copy(a2_ref.at[rows], a2_out.at[rows], row_sem.at[1, i]),
        ])
    fetch = pltpu.make_async_copy(tokens_ref.at[place.t], x_ref, local_sem.at[2])

    def relay_z(copies):
        recv(copies[1])
        start(copies[2])

    def pass_own(seg):
        recv(seg.z[0], seg.z[2])
        if seg is segw:
            start(seg.first)
        start(seg.second[0], seg.core[0])

    def pass_second(seg):
        recv(seg.second)
        if seg is seg2:
            start(seg.core[1])

    def pass_first(seg):
        recv(seg.first)
        if seg is segw:
            start(seg.second[1], seg.core[1])
        else:
            start(seg.far[1], seg.far[0])

    def pass_far(seg):
        recv(seg.far[0], seg.far[2])
        start(seg.core[1:] if seg is seg1 else [])

    def pass_core(seg, i):
        recv(seg.second[i])
        start(seg.core[2 + i])

    plan = [
        (0, 0, lambda: (pass_own(segw), pass_first(seg1), relay_z(seg2.z), pass_first(seg2))),
        (0, 3, lambda: (pass_first(segw), relay_z(seg1.z), pass_core(seg0, 0))),
        (1, 0, lambda: recv(seg0.core[:2])),
        (1, 1, lambda: relay_z(seg1.far)),
        (1, 3, lambda: pass_core(seg0, 1)),
        (1, 4, lambda: (recv(segw.core[:2]), pass_core(segw, 0), pass_own(seg2))),
        (2, 1, lambda: relay_z(seg2.far)),
        (2, 2, lambda: pass_core(segw, 1)),
        (2, 3, lambda: pass_own(seg1)),
        (3, 0, lambda: (recv(seg0.core[2:]), pass_far(seg1), flush[0][0].start())),
        (3, 2, lambda: (pass_second(seg2), flush[1][0].start())),
        (3, 3, lambda: (pass_far(seg2), flush[1][2].start())),
        (3, 4, lambda: recv(segw.core[2:])),
    ]

    def serve(point):
        for step, where, act in plan:
            if where == point:
                pl.when(t == step)(lambda act=act: (act(), None)[1])

    @pl.when(t == 0)
    def _():
        s0, s1, s2, s3 = tie_ref[0], tie_ref[1], tie_ref[2], tie_ref[3]
        fetch.start()
        square_ref[...] = jnp.zeros_like(square_ref)
        gain = gains_ref.shape[-1]
        square_ref[0:1, :gain] = gains_ref[s0].astype(F32)[0:1]
        square_ref[1:2, :gain] = gains_ref[s2].astype(F32)[1:2]
        kinds = [s0, s0, s0, s1, s2, s3, s2, s2, s2, s2]
        for i, source in enumerate(kinds):
            wide = bias_ref[i].astype(F32)
            here = lax.broadcasted_iota(jnp.int32, wide.shape, 0) == source
            square_ref[2 + i : 3 + i, :gain] = jnp.sum(
                jnp.where(here, wide, 0.0), 0, keepdims=True
            )
        vec_ref[...] = square_ref[...].T[:gain]
        for j in range(3):
            own0_ref[:, j * width : (j + 1) * width] = in_ref[s0, j]
        place.greet(place.same_t + place.same_dp)
        start(vec_one, seg0.z[1], seg0.z[0], seg0.first[0])
        vecs_ref[z, y, x, c] = vec_ref[...]
        ones = lax.broadcasted_iota(jnp.int32, (vt_ref.shape[1] - HEAD_DIM, n), 0) == 0
        for h in range(heads):
            vt_ref[h, HEAD_DIM:, :] = ones.astype(BF16)
        all0_ref[0, z, y] = own0_ref[...]
        ownw_ref[...] = out_ref[s1].T
        allw_ref[0, z, y] = ownw_ref[...]
        own1_ref[...] = expand_ref[s2]
        own2_ref[...] = project_ref[s3]
        w1_ref[0, z, y] = own1_ref[...]
        w2_ref[0, z, y] = own2_ref[...]
        recv(vec_one)
        start(vec_two)
        relay_z(seg0.z)
        start(seg0.first[2])
        recv(seg0.z[0])
        start(seg0.first[1], segw.z[1], segw.z[0], seg2.z[1])
        recv(vec_two)
        start(seg2.first)
        vecs = vecs_ref[...].reshape(D, vecs_ref.shape[-1]).T[:16]
        rows_ref[...] = vecs
        recv(seg0.z[2])
        start(seg0.first[3], seg1.first, seg0.second[0], seg0.core[0])
        for k in range(4):
            part = slice(k * width, (k + 1) * width)
            bqv_ref[k, 0:1, :width] = vecs[3:4, part]
            bqv_ref[k, 0:1, width : 2 * width] = jnp.zeros((1, width), F32)
            bqv_ref[k, 0:1, 2 * width :] = vecs[4:5, part]
        fetch.wait()

        @pl.loop(0, n // step)
        def _(b):
            rows = pl.ds(pl.multiple_of(b * step, step), step)
            wide = x_ref[rows, :].astype(F32)
            xhat, _ = norm_parts(wide)
            a1 = (xhat * rows_ref[0:1, :] + rows_ref[2:3, :]).astype(BF16)
            a1_ref[rows, :] = a1
            a1t_ref[:, rows] = a1.T
            h1_ref[rows, :] = wide + rows_ref[5:6, :]

        put_a1t.start()
        relay_z(segw.z)
        start(seg2.z[0], seg1.z[1], seg1.z[0])
        recv(seg0.first)
        start(seg0.second[1], seg0.core[1])

    serve(0)
    gq = all0_ref[t].reshape(D, 3 * width)
    gq_ref[0] = gq
    mine = place.group(t)
    qkv = dot_nn(a1_ref[...], gq) + bqv_ref[mine, 0:1, :]
    q = qkv[:, :width].astype(BF16) * jnp.asarray(HEAD_DIM ** -0.5, BF16)
    k = qkv[:, width : 2 * width].astype(BF16)
    v = qkv[:, 2 * width :].astype(BF16)
    q_ref[0] = q
    kt_ref[0] = k.T
    v_ref[0] = v
    vt = v.T
    for h in range(heads):
        vt_ref[h, :HEAD_DIM, :] = vt[h * HEAD_DIM : (h + 1) * HEAD_DIM]
    spare = k_ref.shape[1] - width
    dead = lax.broadcasted_iota(jnp.int32, (n, spare), 0) >= length
    first_column = lax.broadcasted_iota(jnp.int32, (n, spare), 1) == 0
    k_ref[:, :width] = k
    k_ref[:, width:] = jnp.where(first_column & dead, MASKED, 0.0).astype(BF16)
    qa_ref[:, :width] = q
    qa_ref[:, width:] = jnp.where(first_column, 1.0, 0.0).astype(BF16)

    serve(1)
    def scores(h, b):
        first, last = b * step, (b + 1) * step
        q = qa_ref[first:last, :]
        lane = lax.broadcasted_iota(jnp.int32, (1, q.shape[1]), 1)
        keep = head_mask((1, q.shape[1]), h) | (lane >= width)
        return dot_nt(k_ref[:last, :], jnp.where(keep, q, jnp.zeros((), BF16)))

    def attend(h, b, s):
        first, last = b * step, (b + 1) * step
        key = lax.broadcasted_iota(jnp.int32, (step, step), 0)
        query = lax.broadcasted_iota(jnp.int32, (step, step), 1)
        near = jnp.where(key <= query, s[first:], MASKED)
        top = jnp.max(near, 0, keepdims=True)
        if b:
            far = s[:first]
            top = jnp.maximum(top, jnp.max(far, 0, keepdims=True))
        e_near = jnp.exp((near - top).astype(BF16))
        p_ref[0, h, b, first:last, :] = e_near
        o = dot_nn(vt_ref[h, :, first:last], e_near)
        if b:
            e_far = jnp.exp((far - top).astype(BF16))
            p_ref[0, h, b, :first, :] = e_far
            o += dot_nn(vt_ref[h, :, :first], e_far)
        scale = 1.0 / o[HEAD_DIM : HEAD_DIM + 1]
        scale_ref[0, h : h + 1, first:last] = scale
        ot_ref[h * HEAD_DIM : (h + 1) * HEAD_DIM, first:last] = (
            o[:HEAD_DIM] * scale
        ).astype(BF16)

    scale_ref[0, heads:, :] = jnp.zeros((scale_ref.shape[1] - heads, n), F32)
    for h in range(heads):
        s = scores(h, 0)
        for b in range(n // step):
            ahead = scores(h, b + 1) if b + 1 < n // step else None
            attend(h, b, s)
            s = ahead
        serve(2 + h)

    gw_ref[0] = allw_ref[t].reshape(gw_ref.shape[1:])
    o = ot_ref[...].T
    o_ref[0] = o
    h1_ref[...] += dot_nt(o, gw_ref[0])

    @pl.when(t == 3)
    def _():
        for i, rows in enumerate(blocks(n, step)):
            xhat, _ = norm_parts(h1_ref[rows, :])
            a2 = (xhat * rows_ref[1:2, :] + rows_ref[6:7, :]).astype(BF16)
            a2_ref[rows, :] = a2
            a2t_ref[:, rows] = a2.T
            for put in puts[i]:
                put.start()
        put_a2t.start()
        recv(seg2.core)
        flush[1][1].start()
        recv(seg1.core)
        flush[0][1].start()
        pass_second(seg1)
        flush[0][2].start()
        links.sent()
        for copies in flush + puts + [[put_a1t, put_a2t]]:
            for copy in copies:
                copy.wait()


N_GATHER = 10 + 13 + 10 + 10 + 10
VMEM_WHOLE = pl.BlockSpec(memory_space=pltpu.VMEM)
ANY_WHOLE = pl.BlockSpec(memory_space=pl.ANY)


def run_fused_forward(tie, lengths, tokens, gains, biases, w_in, w_out, w_expand, w_project):
    groups, n, _ = tokens.shape
    depth, width = w_in.shape[-2:]
    heads = width // HEAD_DIM
    hidden = w_expand.shape[-1]
    w_project = w_project.transpose(0, 2, 1)
    biases = biases.transpose(1, 0, 2)
    own = gains.shape[-1]
    return pl.pallas_call(
        fused_forward,
        grid=(groups,),
        in_specs=[SMEM_WHOLE, SMEM_WHOLE, ANY_WHOLE] + [VMEM_WHOLE] * 6,
        out_specs=[
            group(D, 3 * width), group(D, width), ANY_WHOLE, ANY_WHOLE, VMEM_WHOLE,
            group(n, width), group(n, width), group(width, n), group(heads, n // 256, n, 256),
            group(8, n), group(n, width), ANY_WHOLE, ANY_WHOLE, ANY_WHOLE, ANY_WHOLE,
        ],
        out_shape=[
            shaped(BF16, groups, D, 3 * width), shaped(BF16, groups, D, width),
            shaped(BF16, groups, Z_DEV, Y_DEV, depth, hidden),
            shaped(BF16, groups, Z_DEV, Y_DEV, depth, hidden),
            shaped(F32, 16, D),
            shaped(BF16, groups, n, width), shaped(BF16, groups, n, width),
            shaped(BF16, groups, width, n), shaped(BF16, groups, heads, n // 256, n, 256),
            shaped(F32, groups, 8, n), shaped(BF16, groups, n, width), shaped(BF16, D, n), shaped(F32, n, D),
            shaped(BF16, n, D), shaped(BF16, D, n),
        ],
        scratch_shapes=[
            pltpu.VMEM((depth, 3 * width), BF16), pltpu.VMEM((depth, width), BF16),
            pltpu.VMEM((depth, hidden), BF16), pltpu.VMEM((depth, hidden), BF16),
            pltpu.VMEM((128, 128), F32), pltpu.VMEM((own, 128), F32),
            pltpu.VMEM((groups, Z_DEV, Y_DEV, depth, 3 * width), BF16),
            pltpu.VMEM((groups, Z_DEV, Y_DEV, depth, width), BF16),
            pltpu.VMEM((groups, Z_DEV, Y_DEV, depth, hidden), BF16),
            pltpu.VMEM((groups, Z_DEV, Y_DEV, depth, hidden), BF16),
            pltpu.VMEM((Z_DEV, Y_DEV, X_DEV, C_DEV, own, 128), F32),
            pltpu.VMEM((groups, 8, 3 * width), F32),
            pltpu.VMEM((n, D), BF16), pltpu.VMEM((n, D), BF16), pltpu.VMEM((n, 256), BF16),
            pltpu.VMEM((n, 256), BF16), pltpu.VMEM((heads, HEAD_DIM + 16, n), BF16),
            pltpu.VMEM((width, n), BF16),
            pltpu.VMEM((D, n), BF16), pltpu.VMEM((n, D), F32), pltpu.VMEM((n, D), BF16),
            pltpu.VMEM((D, n), BF16),
            pltpu.SemaphoreType.DMA((N_GATHER,)), pltpu.SemaphoreType.DMA((N_GATHER,)),
            pltpu.SemaphoreType.DMA((3,)), pltpu.SemaphoreType.DMA((2, 4)),
            pltpu.SemaphoreType.DMA((2, n // 256)),
        ],
        compiler_params=pltpu.CompilerParams(
            vmem_limit_bytes=VMEM_LIMIT, collective_id=0, has_side_effects=True
        ),
        name="fused_forward",
    )(tie, lengths, tokens, gains, biases, w_in, w_out, w_expand, w_project)


class Result:
    def __init__(self, links, place, own_ref, passing_ref, out_ref, step, sem, count):
        self.x, self.core, self.far, self.keep, self.keep_far = [], [], [], [], []
        for i in range(count):
            rows = pl.ds(i * step, step)
            mine, theirs = out_ref.at[place.t, rows], out_ref.at[place.ts[2], rows]
            own, passing = own_ref.at[rows], passing_ref.at[rows]
            self.x.append(links.add(place.to_x, own, passing))
            self.core.append(links.add(place.to_core, own, mine))
            self.far.append(links.add(place.to_core, passing, theirs))
            self.keep.append(pltpu.make_async_copy(own, mine, sem.at[0, i]))
            self.keep_far.append(pltpu.make_async_copy(passing, theirs, sem.at[1, i]))

    def send(self, i):
        start(self.x[i], self.core[i], self.keep[i])

    def pass_on(self, i):
        recv(self.x[i])
        start(self.far[i], self.keep_far[i])

    def finish(self):
        recv(self.core, self.far)
        for copy in self.keep + self.keep_far:
            copy.wait()


def low(value):
    return jnp.asarray(value, BF16)


def pair_order(i):
    return i + 1 - 2 * (i % 2)


def fused_feed_forward(
    len_ref, cot_ref, a2_ref, a2t_in, h1_in, far1_ref, far2_ref, rows_ref,
    out_out, fold_ref, work_out, dh1_out, gb_out, gbt_out, sums_ref,
    gf_ref, gft_ref, feed_ref, da2_ref, h_ref, df_ref, weights_ref, missing_ref, third_ref, late_ref,
    stage_ref, land_ref, near_ref, cross_ref, a2t_ref, h1_ref, out_ref, work_ref,
    send_sem, recv_sem, local_sem, row_sem,
):
    t = pl.program_id(0)
    n = gf_ref.shape[0]
    step = 256
    depth = stage_ref.shape[-2]
    place = Place()
    length = len_ref[place.t]
    links = Links(send_sem, recv_sem)
    y, other = place.y, place.other_y
    last = [
        links.add(place.to_x, far1_ref.at[0, :, other], missing_ref.at[0, 0]),
        links.add(place.to_y, far2_ref.at[2, :, y], missing_ref.at[1, 0]),
    ]
    last_core = [
        links.add(place.to_core, missing_ref.at[i, 0], missing_ref.at[i, 1]) for i in range(2)
    ]
    there, to_come = pl.ds(0, Z_DEV // 2), pl.ds(Z_DEV // 2, Z_DEV // 2)
    third = [
        links.add(place.to_core, far1_ref.at[2, there, y], third_ref.at[0, there]),
        links.add(place.to_core, far2_ref.at[2, :, y], third_ref.at[1]),
    ]
    last.append(links.add(place.to_x, far1_ref.at[0, to_come, y], late_ref))
    last_core.append(links.add(place.to_core, late_ref, third_ref.at[0, to_come]))
    core = [
        [links.add(place.to_core, stage_ref.at[i], land_ref.at[s, i]) for i in range(2)]
        for s in range(2)
    ]
    cross = [
        links.add(place.to_y, near_ref.at[i, :, other], cross_ref.at[i]) for i in range(2)
    ]
    fetch = pltpu.make_async_copy(cot_ref.at[place.t], gf_ref, local_sem.at[0])
    gb_ref, gbt_ref, dh1_ref = gf_ref, gft_ref, da2_ref
    late = [
        pltpu.make_async_copy(a2t_in, a2t_ref, local_sem.at[5]),
        pltpu.make_async_copy(h1_in, h1_ref, local_sem.at[6]),
    ]
    puts = []
    for i in range(n // step):
        rows = pl.ds(i * step, step)
        puts.append([
            pltpu.make_async_copy(ref.at[rows], out.at[rows], row_sem.at[j, i])
            for j, (ref, out) in enumerate(
                [(out_ref, out_out), (dh1_ref, dh1_out), (gb_ref, gb_out)]
            )
        ])
    put_gbt = pltpu.make_async_copy(gbt_ref, gbt_out, local_sem.at[7])
    put_work = pltpu.make_async_copy(work_ref, work_out, local_sem.at[8])
    k = pair_order(t)
    mine = place.group(k)

    def load(step, whole, slot):
        for i, far_ref in enumerate([far1_ref, far2_ref]):
            group = far_ref.at[pair_order(step)]
            to = weights_ref.at[slot, i]
            if not whole:
                group, to = group.at[:, y], to.at[:, y]
            yield pltpu.make_async_copy(group, to, local_sem.at[1 + 2 * slot + i])

    def live_rows(b):
        at = b * step + lax.broadcasted_iota(jnp.int32, (step, 1), 0)
        return (at < length).astype(F32)

    @pl.when(t == 0)
    def _():
        fetch.start()
        for copy in load(0, True, 0):
            copy.start()
        for copy in late:
            copy.start()
        place.greet()
        start(last, third)
        sums_ref[...] = jnp.zeros_like(sums_ref)
        feed_ref[...] = jnp.zeros_like(feed_ref)
        da2_ref[...] = jnp.zeros_like(da2_ref)
        fetch.wait()

        @pl.loop(0, n // step)
        def _(b):
            rows = pl.ds(pl.multiple_of(b * step, step), step)
            g = (gf_ref[rows, :].astype(F32) * live_rows(b)).astype(BF16)
            gf_ref[rows, :] = g
            gft_ref[:, rows] = g.T
            sums_ref[7:8, :] += jnp.sum(g.astype(F32), 0, keepdims=True)

    for i in range(4):
        @pl.when(t == i)
        def _():
            if i == 2:
                recv(last_core, third)
            else:
                for copy in load(i, i < 2, i % 2):
                    copy.wait()
            if i in (0, 2):
                for copy in load(i + 1, i + 1 < 2, (i + 1) % 2):
                    copy.start()
            for j in range(2):
                if i == 2:
                    weights_ref[0, j, :, y] = third_ref[j]
                if i >= 2:
                    weights_ref[i % 2, j, :, other] = missing_ref[j, 3 - i]
            if i == 3:
                weights_ref[1, 0, to_come, y] = late_ref[...]

    bias = rows_ref[pl.ds(8 + mine, 1), :]
    w1 = weights_ref[t % 2, 0].reshape(D, -1)
    w2 = weights_ref[t % 2, 1].reshape(D, -1)
    column = jnp.zeros((1, w1.shape[1]), F32)
    for rows in blocks(n, step):
        f = (dot_nn(a2_ref[rows, :], w1) + bias).astype(BF16)
        dh = dot_nn(gf_ref[rows, :], w2)
        f2 = f * f
        th = jnp.tanh(f * (low(SQRT_2_PI) + low(SQRT_2_PI * 0.044715) * f2))
        half = low(0.5) + low(0.5) * th
        h = f * half
        slope = half + f * (low(0.5) - low(0.5) * th * th) * (
            low(SQRT_2_PI) + low(3 * SQRT_2_PI * 0.044715) * f2
        )
        df = (dh * slope.astype(F32)).astype(BF16)
        h_ref[rows, :] = h
        df_ref[rows, :] = df
        column += jnp.sum(df.astype(F32), 0, keepdims=True)
        feed_ref[rows, :] += dot_nt(h, w2)
        da2_ref[rows, :] += dot_nt(df, w1)
    sums_ref[pl.ds(8 + mine, 1), :] = column

    @pl.when(t == 1)
    def _():
        recv(last)
        start(last_core)

    @pl.when(t == 0)
    def _():
        late[0].wait()

    def weight_grad(left_ref, right_ref):
        value = dot_nn(left_ref[...], right_ref[...])
        return value.reshape(Z_DEV, Y_DEV, depth, value.shape[-1]).astype(BF16)

    grad1 = weight_grad(a2t_ref, df_ref)
    grad2 = weight_grad(gft_ref, h_ref)

    def put(ref):
        ref[0] = grad1
        ref[1] = grad2

    def reduced(ref):
        return lambda i, s, z: (
            ref[i, z].astype(F32) + land_ref[s, i, z].astype(F32)
        ).astype(BF16)

    @pl.when(t == 0)
    def _():
        put(stage_ref)
        start(core[0])

    @pl.when(t == 1)
    def _():
        put(near_ref)
        recv(core[0])

        @pl.loop(0, Z_DEV)
        def _(z):
            for i in range(2):
                near_ref[i, z] = reduced(near_ref)(i, 0, z)

        start(cross)

    @pl.when(t == 2)
    def _():
        for copy in core[0]:
            copy.wait_send()
        put(stage_ref)
        start(core[1])

    @pl.when(t == 3)
    def _():
        put(work_ref)
        late[1].wait()
        for i, rows in enumerate(blocks(n, step)):
            live = live_rows(i)
            h1 = h1_ref[rows, :]
            out_ref[rows, :] = (live * (h1 + (feed_ref[rows, :] + rows_ref[7:8, :]))).astype(BF16)
            xhat, r = norm_parts(h1)
            da2 = da2_ref[rows, :]
            sums_ref[1:2, :] += jnp.sum(da2 * xhat, 0, keepdims=True)
            sums_ref[6:7, :] += jnp.sum(da2, 0, keepdims=True)
            dg = da2 * rows_ref[1:2, :]
            dv = r * (
                dg
                - jnp.mean(dg, -1, keepdims=True)
                - xhat * jnp.mean(dg * xhat, -1, keepdims=True)
            )
            dh1 = gf_ref[rows, :].astype(F32) + dv
            dh1_ref[rows, :] = dh1
            gb = dh1.astype(BF16)
            gb_ref[rows, :] = gb
            gbt_ref[:, rows] = gb.T
            sums_ref[5:6, :] += jnp.sum(gb.astype(F32), 0, keepdims=True)
            for copy in puts[i]:
                copy.start()
        put_gbt.start()
        recv(core[1])

        @pl.loop(0, Z_DEV)
        def _(z):
            for i in range(2):
                work_ref[i, z] = reduced(work_ref)(i, 1, z)

        put_work.start()
        recv(cross)

        @pl.loop(0, Z_DEV)
        def _(z):
            for i in range(2):
                fold_ref[i, z] = (
                    near_ref[i, z, y].astype(F32) + cross_ref[i, z].astype(F32)
                ).astype(BF16)

        links.sent(*core[0])
        for copies in puts + [[put_gbt, put_work]]:
            for copy in copies:
                copy.wait()


def run_fused_feed_forward(lengths, cot, a2, a2t, h1, g1, g2, rows):
    n = cot.shape[1]
    groups, _, _, depth, hidden = g1.shape
    both = (2, Z_DEV, Y_DEV, depth, hidden)
    fold = (2, Z_DEV, depth, hidden)
    return pl.pallas_call(
        fused_feed_forward,
        grid=(groups,),
        in_specs=[SMEM_WHOLE, ANY_WHOLE, VMEM_WHOLE] + [ANY_WHOLE] * 4 + [VMEM_WHOLE],
        out_specs=[ANY_WHOLE, VMEM_WHOLE] + [ANY_WHOLE] * 4 + [VMEM_WHOLE],
        out_shape=[
            shaped(BF16, n, D), shaped(BF16, *fold), shaped(BF16, *both), shaped(F32, n, D),
            shaped(BF16, n, D), shaped(BF16, D, n), shaped(F32, 16, D),
        ],
        scratch_shapes=[
            pltpu.VMEM((n, D), BF16), pltpu.VMEM((D, n), BF16), pltpu.VMEM((n, D), F32),
            pltpu.VMEM((n, D), F32), pltpu.VMEM((n, hidden), BF16), pltpu.VMEM((n, hidden), BF16),
            pltpu.VMEM((2,) + both, BF16),
            pltpu.VMEM((2,) + fold, BF16), pltpu.VMEM(fold, BF16),
            pltpu.VMEM((Z_DEV // 2, depth, hidden), BF16), pltpu.VMEM(both, BF16),
            pltpu.VMEM((2,) + both, BF16),
            pltpu.VMEM(both, BF16), pltpu.VMEM(fold, BF16),
            pltpu.VMEM((D, n), BF16), pltpu.VMEM((n, D), F32), pltpu.VMEM((n, D), BF16),
            pltpu.VMEM(both, BF16),
            pltpu.SemaphoreType.DMA((14,)), pltpu.SemaphoreType.DMA((14,)),
            pltpu.SemaphoreType.DMA((9,)), pltpu.SemaphoreType.DMA((3, n // 256)),
        ],
        compiler_params=pltpu.CompilerParams(
            vmem_limit_bytes=VMEM_LIMIT, collective_id=1, has_side_effects=True
        ),
        name="fused_feed_forward",
    )(lengths, cot, a2, a2t, h1, g1, g2, rows)
class Reduce:
    def __init__(
        self, links, place, work, acc, cross_ref, far_ref, mid_ref, last_ref, side_ref,
        slots=(0, 1), split=False,
    ):
        self.place, self.work, self.acc = place, work, acc
        self.cross_ref, self.far_ref, self.mid_ref = cross_ref, far_ref, mid_ref
        self.last_ref, self.side_ref = last_ref, side_ref
        self.two = len(slots) == 2
        zs = place.zs
        self.y = {
            s: [
                links.add(
                    place.to_y, work(s, zs[j], place.other_y),
                    cross_ref.at[s if self.two else 0, zs[j]],
                )
                for j in (1, 3, 2, 0)
            ]
            for s in slots
        }
        self.z = [
            [
                links.add(place.to_z[1], acc(s, zs[1]), far_ref.at[s, 0]),
                links.add(place.to_z[1], acc(s, zs[3]), far_ref.at[s, 1]),
                links.add(place.to_z[2], mid_ref.at[s, 1], far_ref.at[s, 2]),
            ]
            for s in range(1 if split else 2)
        ]
        self.x = links.add(place.to_x, last_ref, side_ref)

    def fold_y(self, s, half):
        for i, j in [(0, 1), (1, 3), (2, 2), (3, 0)][2 * half : 2 * half + 2]:
            z = self.place.zs[j]
            recv(self.y[s][i])
            value = self.work(s, z, self.place.y)[...].astype(F32)
            cross = self.cross_ref[s if self.two else 0, z].astype(F32)
            self.acc(s, z)[...] = (value + cross).astype(BF16)
            if i < 2:
                start(self.z[s][i])

    def fold_z(self, s):
        recv(self.z[s][:2])
        for i in (1, 0):
            value = self.acc(s, self.place.zs[2 * i])[...].astype(F32)
            self.mid_ref[s, i] = (value + self.far_ref[s, i].astype(F32)).astype(BF16)
            if i:
                start(self.z[s][2])

    def own(self, s):
        recv(self.z[s][2])
        return self.mid_ref[s, 0].astype(F32) + self.far_ref[s, 2].astype(F32)

    def send_x(self):
        self.last_ref[...] = self.own(1).astype(BF16)
        start(self.x)

    def total(self):
        value = self.own(0)
        recv(self.x)
        return value + self.side_ref[...].astype(F32)


class ReduceHalves:
    def __init__(self, links, place, work, landings, last_ref):
        self.place, self.work = place, work
        self.cross, self.far, self.mid, self.far2, self.mid2, self.fin2, self.cross2 = landings
        self.last_ref = last_ref
        zs, half = place.zs, last_ref.shape[0] // 2
        self.low, self.high = pl.ds(0, half), pl.ds(half, half)
        every = slice(None)
        y, other = place.y, place.other_y
        self.y = [
            links.add(place.to_y, work.at[zs[j], other, self.low], self.cross.at[zs[j]])
            for j in (1, 3, 2, 0)
        ]
        self.z = [
            links.add(place.to_z[1], work.at[zs[1], y, self.low], self.far.at[0]),
            links.add(place.to_z[1], work.at[zs[3], y, self.low], self.far.at[1]),
            links.add(place.to_z[2], self.mid.at[1], self.far.at[2]),
        ]
        self.z2 = [
            links.add(place.to_z[1], work.at[zs[1], every, self.high], self.far2.at[0]),
            links.add(place.to_z[1], work.at[zs[3], every, self.high], self.far2.at[1]),
            links.add(place.to_z[2], self.mid2.at[1], self.far2.at[2]),
        ]
        self.y2 = links.add(place.to_y, self.fin2.at[other], self.cross2)

    def begin(self):
        start(self.y, self.z2[:2])

    def add(self, target, left, right):
        target[...] = (left[...].astype(F32) + right[...].astype(F32)).astype(BF16)

    def fold_y(self):
        y, zs = self.place.y, self.place.zs
        for i, j in enumerate((1, 3, 2, 0)):
            recv(self.y[i])
            block = self.work.at[zs[j], y, self.low]
            self.add(block, block, self.cross.at[zs[j]])
            if i < 2:
                start(self.z[i])

    def fold_high(self):
        recv(self.z2[:2])
        for i in (1, 0):
            block = self.work.at[self.place.zs[2 * i], :, self.high]
            self.add(self.mid2.at[i], block, self.far2.at[i])
            if i:
                start(self.z2[2])

    def cross_high(self):
        recv(self.z2[2])
        self.add(self.fin2, self.mid2.at[0], self.far2.at[2])
        start(self.y2)

    def fold_z(self):
        recv(self.z[:2])
        for i in (1, 0):
            block = self.work.at[self.place.zs[2 * i], self.place.y, self.low]
            self.add(self.mid.at[i], block, self.far.at[i])
            if i:
                start(self.z[2])

    def finish(self):
        recv(self.z[2])
        self.add(self.last_ref.at[self.low], self.mid.at[0], self.far.at[2])
        recv(self.y2)
        self.add(self.last_ref.at[self.high], self.fin2.at[self.place.y], self.cross2)


def fused_backward(
    tokens_ref, gq_in, gw_in, rows_ref, dh1_ref, gb_ref, gbt_in, q_in, v_in, kt_in,
    p_ref, scale_in, o_in, a1t_in, layer_in, fold_in, work_in, early_ref,
    out_ref, layerout_ref, part0_ref, partw_ref, part1_ref, part2_ref, total_ref,
    gq_ref, gw_ref, q_ref, v_ref, kt_ref, scale_ref, o_ref,
    a1t_ref, gbt_ref, layer_ref, fold_ref, work_ref, do_ref, delta_ref, dkv_ref, dqkv_ref, da1_ref, own_ref, passing_ref, passlayer_ref, bqv_ref,
    folded_ref, cross1_ref, far1_ref, mid1_ref, last1_ref, side1_ref,
    cross2_ref, far2_ref, mid2_ref, last2_ref, side2_ref,
    stagew_ref, landw_ref, workw_ref, crossw_ref, farw_ref, midw_ref, lastw_ref, sidew_ref,
    stage0_ref, land0_ref, work0_ref, cross0_ref, far0_ref, mid0_ref, last0_ref, side0_ref,
    sums_ref, sumland_ref,
    send_sem, recv_sem, local_sem, result_sem, group_sem, *tail_refs,
):
    t = pl.program_id(0)
    n = own_ref.shape[0]
    width = gw_ref.shape[-1]
    depth = part0_ref.shape[0]
    heads = width // HEAD_DIM
    step = n // 4
    place = Place()
    y = place.y
    links = Links(send_sem, recv_sem)
    k, i = group_and_block(t)
    mine = place.group(k)
    now = k % 2
    out = Result(links, place, own_ref, passing_ref, out_ref, step, result_sem.at[0], 4)
    layer = Result(links, place, layer_ref, passlayer_ref, layerout_ref, step, result_sem.at[1], 4)
    fetch = pltpu.make_async_copy(tokens_ref.at[place.t], own_ref, local_sem.at[0])
    fetch_layer, fetch_work, fetch_fold, fetch_gbt, fetch_a1t = [
        pltpu.make_async_copy(there, here, local_sem.at[1 + j])
        for j, (there, here) in enumerate([
            (layer_in, layer_ref), (work_in, work_ref), (fold_in, fold_ref),
            (gbt_in, gbt_ref), (a1t_in, a1t_ref),
        ])
    ]
    def operands(group):
        slot = group % 2
        pairs = [
            (gw_in, gw_ref), (scale_in, scale_ref), (o_in, o_ref), (v_in, v_ref),
            (q_in, q_ref), (kt_in, kt_ref), (gq_in, gq_ref),
        ]
        return [
            pltpu.make_async_copy(there.at[group], here.at[slot], group_sem.at[slot, j])
            for j, (there, here) in enumerate(pairs)
        ]

    corew = [links.add(place.to_core, stagew_ref, landw_ref.at[i]) for i in range(2)]
    core0 = [links.add(place.to_core, stage0_ref, land0_ref.at[i]) for i in range(2)]
    def half_done(i, *landing):
        return Reduce(
            links, place, lambda s, z, y: work_ref.at[i, z, y],
            lambda s, z: folded_ref.at[i, z] if s else fold_ref.at[i, z],
            *landing, slots=(1,),
        )

    seg1 = half_done(0, cross1_ref, far1_ref, mid1_ref, last1_ref, side1_ref)
    seg2 = half_done(1, cross2_ref, far2_ref, mid2_ref, last2_ref, side2_ref)
    segw = Reduce(
        links, place, lambda s, z, y: workw_ref.at[s, z, y],
        lambda s, z: workw_ref.at[s, z, y],
        crossw_ref, farw_ref, midw_ref, lastw_ref, sidew_ref,
    )
    seg0 = Reduce(
        links, place, lambda s, z, y: work0_ref.at[s, z, y],
        lambda s, z: work0_ref.at[s, z, y],
        cross0_ref, far0_ref, mid0_ref, last0_ref, side0_ref, slots=(0,), split=True,
    )
    tail = ReduceHalves(links, place, work0_ref.at[1], tail_refs, last0_ref)
    sum_core, sum_y, *sum_z, sum_x = [
        links.add(to, sums_ref.at[i], sumland_ref.at[j])
        for j, (i, to) in enumerate(
            zip([0, 1, 2, 2, 2, 3], [place.to_core, place.to_y] + place.to_z[1:] + [place.to_x])
        )
    ]

    early_copies = [
        corew[1], core0[1], *segw.y[0], *segw.y[1], *segw.z[0], *seg0.y[0], *seg0.z[0],
        out.x[3], out.core[3], *layer.x, *layer.core, *layer.far, seg1.x, seg2.x,
    ]
    for seg in (seg1, seg2):
        early_copies += [*seg.y[1], *seg.z[0], *seg.z[1]]

    def sent(copies):
        for copy in copies:
            copy.wait_send()

    def when(point):
        return pl.when(t == point)

    @when(0)
    def _():
        start(fetch_layer, operands(1), fetch_work, fetch_fold, fetch_gbt, operands(0))
        start(fetch, fetch_a1t)
        place.greet()
        fetch_layer.wait()
        for i in range(4):
            layer.send(i)
        fetch_work.wait()
        start(seg1.y[1], seg2.y[1])
        fetch_fold.wait()
        start(seg1.z[0][:2], seg2.z[0][:2])
        bqv_ref[...] = jnp.zeros_like(bqv_ref)
        sums_ref[0] = early_ref[...]
        fetch_gbt.wait()

    def add_core():
        recv(corew[1])

        @pl.loop(0, Z_DEV)
        def _(z):
            workw_ref[1, z] = (
                workw_ref[1, z].astype(F32) + landw_ref[1, z].astype(F32)
            ).astype(BF16)

        start(segw.y[1])

    def wait(copies):
        for copy in copies:
            copy.wait()

    @when(0)
    def _():
        wait(operands(1))

    @when(4)
    def _():
        start(operands(3))
        wait(operands(0))

    @when(8)
    def _():
        start(operands(2))
        wait(operands(3))

    @when(9)
    def _():
        wait(operands(2))

    plan = [
        (2, 1, lambda: (seg1.fold_y(1, 0), seg1.fold_z(0))),
        (3, 1, lambda: layer.pass_on(0)),
        (4, 0, lambda: (seg1.fold_y(1, 1), seg2.fold_z(0))),
        (4, 1, lambda: layer.pass_on(1)),
        (5, 1, lambda: (seg1.fold_z(1), seg2.fold_y(1, 0))),
        (8, 0, lambda: (seg2.fold_y(1, 1), layer.pass_on(2))),
        (8, 1, lambda: (seg1.send_x(), segw.fold_y(0, 0), segw.fold_y(0, 1))),
        (9, 0, add_core),
        (9, 1, lambda: (seg2.fold_z(1), seg0.fold_y(0, 0), layer.pass_on(3))),
        (10, 1, lambda: segw.fold_z(0)),
        (11, 1, lambda: (seg2.send_x(), seg0.fold_y(0, 1))),
        (12, 1, lambda: (segw.fold_y(1, 0), segw.fold_y(1, 1))),
        (13, 1, lambda: (seg0.fold_z(0), out.pass_on(3))),
        (14, 1, lambda: segw.fold_z(1)),
    ]

    def serve(point):
        for at, where, act in plan:
            if where == point:
                pl.when(t == at)(lambda act=act: (act(), None)[1])

    @pl.when((t == 0) | (t == 4) | (t == 8) | (t == 9))
    def _():
        pick = (
            lax.broadcasted_iota(jnp.int32, (8, width), 1) // HEAD_DIM
            == lax.broadcasted_iota(jnp.int32, (8, width), 0)
        ).astype(BF16)

        @pl.loop(0, n // step)
        def _(i):
            rows = pl.ds(pl.multiple_of(i * step, step), step)
            columns = scale_ref[now, :, rows].T
            lane = lax.broadcasted_iota(jnp.int32, (step, width), 1)
            scale = columns[:, heads - 1 : heads]
            for h in reversed(range(heads - 1)):
                scale = jnp.where(lane < (h + 1) * HEAD_DIM, columns[:, h : h + 1], scale)
            do = (dot_nn(gb_ref[rows, :], gw_ref[now]) * scale).astype(BF16)
            do_ref[now, rows, :] = do
            product = do.astype(F32) * o_ref[now, rows, :].astype(F32)
            high = product.astype(BF16)
            low = (product - high.astype(F32)).astype(BF16)
            delta_ref[now, :, rows] = dot_nt(pick, high) + dot_nt(pick, low)

        value = dot_nn(gbt_ref[...], o_ref[now]).reshape(Z_DEV, Y_DEV, depth, width)
        for s in range(2):
            @when(8 * s)
            def _():
                if s:
                    corew[0].wait_send()
                stagew_ref[...] = value.astype(BF16)
                start(corew[s])

        @when(4)
        def _():
            recv(corew[0])
            workw_ref[0] = (value + landw_ref[0].astype(F32)).astype(BF16)
            start(segw.y[0])

        @when(9)
        def _():
            workw_ref[1] = value.astype(BF16)

    serve(0)

    for ii in reversed(range(4)):
        @pl.when(i == ii)
        def _():
            first, last = ii * step, (ii + 1) * step
            do = do_ref[now, first:last, :]
            q = q_ref[now, first:last, :]
            v = v_ref[now, :last, :]
            lane = lax.broadcasted_iota(jnp.int32, (1, width), 1)
            dk, dv, dq = None, None, []
            for h in range(heads):
                low, high = h * HEAD_DIM, (h + 1) * HEAD_DIM
                here = (lane >= low) & (lane < high)
                p = p_ref[0, h, 0, :last, :]
                dp = dot_nt(v, jnp.where(here, do, jnp.zeros((), BF16)))
                ds = p * (dp - delta_ref[now, h : h + 1, first:last]).astype(BF16)
                part = dot_nn(p, do)
                dv = part if dv is None else jnp.where(lane < low, dv, part)
                part = dot_nn(ds, q)
                dk = part if dk is None else jnp.where(lane < low, dk, part)
                dq.append(dot_nn(kt_ref[now, low:high, :last], ds))
            if ii == 3:
                dkv_ref[now, 0] = dk
                dkv_ref[now, 1] = dv
            else:
                dkv_ref[now, 0, :last, :] += dk
                dkv_ref[now, 1, :last, :] += dv
            dk = dkv_ref[now, 0, first:last, :].astype(BF16)
            dv = dkv_ref[now, 1, first:last, :].astype(BF16)
            dq = (jnp.concatenate(dq, 0) * HEAD_DIM ** -0.5).astype(BF16).T
            dqkv_ref[now, first:last, :width] = dq
            dqkv_ref[now, first:last, width : 2 * width] = dk
            dqkv_ref[now, first:last, 2 * width :] = dv
            bqv_ref[mine, 0:1, :] += jnp.sum(dq.astype(F32), 0, keepdims=True)
            bqv_ref[mine, 1:2, :] += jnp.sum(dv.astype(F32), 0, keepdims=True)

            @pl.when(t >= 8)
            def _():
                da1_ref[first:last, :] += dot_nt(dqkv_ref[now, first:last, :], gq_ref[now])

    serve(1)

    @pl.when((t == 3) | (t == 7) | (t > 13))
    def _():
        @when(3)
        def _():
            fetch.wait()
            fetch_a1t.wait()

        @when(3)
        def _():
            da1_ref[...] = dot_nt(dqkv_ref[now], gq_ref[now])

        @when(7)
        def _():
            da1_ref[...] += dot_nt(dqkv_ref[now], gq_ref[now])

        value = dot_nn(a1t_ref[...], dqkv_ref[now]).reshape(Z_DEV, Y_DEV, depth, 3 * width)
        for s in range(2):
            @when(3 + 11 * s)
            def _():
                if s:
                    core0[0].wait_send()
                stage0_ref[...] = value.astype(BF16)
                start(core0[s])

            @when(7 + 8 * s)
            def _():
                recv(core0[s])
                work0_ref[s] = (value + land0_ref[s].astype(F32)).astype(BF16)
                if s:
                    tail.begin()
                else:
                    start(seg0.y[s])

    @pl.when((t > 8) & (t % 2 == 1))
    def _():
        rows = pl.ds(pl.multiple_of(i * step, step), step)
        xhat, r = norm_parts(own_ref[rows, :].astype(F32))
        da1 = da1_ref[rows, :]
        sums_ref[0, 0:1, :] += jnp.sum(da1 * xhat, 0, keepdims=True)
        sums_ref[0, 2:3, :] += jnp.sum(da1, 0, keepdims=True)
        dg = da1 * rows_ref[0:1, :]
        dv = r * (
            dg
            - jnp.mean(dg, -1, keepdims=True)
            - xhat * jnp.mean(dg * xhat, -1, keepdims=True)
        )
        own_ref[rows, :] = (dh1_ref[...] + dv).astype(BF16)
        for ii in range(4):
            @pl.when(i == ii)
            def _():
                out.send(ii)

    @when(15)
    def _():
        for s in range(4):
            sums_ref[0, 3:5, s * width : (s + 1) * width] = bqv_ref[s, 0:2, :]
        start(sum_core)
        segw.send_x()
        part1_ref[...] = seg1.total()
        part2_ref[...] = seg2.total()
        sent(early_copies)
        tail.fold_high()
        recv(sum_core)
        sums_ref[1] = sums_ref[0] + sumland_ref[0]
        start(sum_y)
        tail.fold_y()
        tail.cross_high()
        tail.fold_z()
        recv(sum_y)
        sums_ref[2] = sums_ref[1] + sumland_ref[1]
        start(sum_z)
        out.pass_on(2)
        tail.finish()
        start(seg0.x)
        recv(sum_z)
        sums_ref[3] = (sums_ref[2] + sumland_ref[2]) + (sumland_ref[3] + sumland_ref[4])
        start(sum_x)
        out.pass_on(1)
        partw_ref[...] = segw.total()
        layer.finish()
        out.pass_on(0)
        recv(sum_x)
        total_ref[...] = sums_ref[3] + sumland_ref[5]
        part0_ref[...] = seg0.total()
        out.finish()
        links.sent(corew[0], core0[0], *early_copies)


def group_and_block(t):
    early = t < 8
    return (
        jnp.where(early, 1 - t // 4, 3 - t % 2),
        3 - jnp.where(early, t % 4, jnp.maximum(t - 8, 0) // 2),
    )


def run_fused_backward(
    tokens, gq, gw, rows, dh1, gb, gbt, q, v, kt, p, scale, o, a1t, layer, fold, work, early
):
    groups, n, _ = tokens.shape
    width = gw.shape[-1]
    heads = width // HEAD_DIM
    hidden = fold.shape[-1]
    depth = D // (Z_DEV * Y_DEV)
    step = n // 4

    p_spec = pl.BlockSpec(
        (1, heads, 1, n, step),
        lambda t: (group_and_block(t)[0], 0, group_and_block(t)[1], 0, 0),
    )

    copies = 12 + 12 + 4 + 15 + 2 * 11 + 8 + 11 + 6

    def landing(lanes, slots=1):
        return [
            pltpu.VMEM((slots, Z_DEV, depth, lanes), BF16),
            pltpu.VMEM((2, 3, depth, lanes), BF16), pltpu.VMEM((2, 2, depth, lanes), BF16),
            pltpu.VMEM((depth, lanes), BF16), pltpu.VMEM((depth, lanes), BF16),
        ]

    def working(lanes):
        block = (Z_DEV, Y_DEV, depth, lanes)
        return [pltpu.VMEM(block, BF16)] + [pltpu.VMEM((2,) + block, BF16)] * 2

    return pl.pallas_call(
        fused_backward,
        grid=(4 * groups,),
        in_specs=[
            ANY_WHOLE, ANY_WHOLE, ANY_WHOLE, VMEM_WHOLE,
            pl.BlockSpec((step, D), lambda t: (group_and_block(jnp.maximum(t, 8))[1], 0)),
            VMEM_WHOLE, ANY_WHOLE, ANY_WHOLE, ANY_WHOLE, ANY_WHOLE, p_spec,
            ANY_WHOLE, ANY_WHOLE, ANY_WHOLE, ANY_WHOLE, ANY_WHOLE, ANY_WHOLE, VMEM_WHOLE,
        ],
        out_specs=[ANY_WHOLE] * 2 + [VMEM_WHOLE] * 5,
        out_shape=[
            shaped(BF16, groups, n, D), shaped(BF16, groups, n, D),
            shaped(F32, depth, 3 * width),
            shaped(F32, depth, width), shaped(F32, depth, hidden),
            shaped(F32, depth, hidden), shaped(F32, 16, D),
        ],
        scratch_shapes=[
            pltpu.VMEM((2, D, 3 * width), BF16), pltpu.VMEM((2, D, width), BF16),
            pltpu.VMEM((2, n, width), BF16), pltpu.VMEM((2, n, width), BF16),
            pltpu.VMEM((2, width, n), BF16), pltpu.VMEM((2, 8, n), F32),
            pltpu.VMEM((2, n, width), BF16),
            pltpu.VMEM((D, n), BF16), pltpu.VMEM((D, n), BF16), pltpu.VMEM((n, D), BF16),
            pltpu.VMEM((2, Z_DEV, depth, hidden), BF16),
            pltpu.VMEM((2, Z_DEV, Y_DEV, depth, hidden), BF16),
            pltpu.VMEM((2, n, width), BF16),
            pltpu.VMEM((2, 8, n), F32), pltpu.VMEM((2, 2, n, width), F32),
            pltpu.VMEM((2, n, 3 * width), BF16), pltpu.VMEM((n, D), F32),
            pltpu.VMEM((n, D), BF16), pltpu.VMEM((n, D), BF16), pltpu.VMEM((n, D), BF16),
            pltpu.VMEM((groups, 8, width), F32),
        ]
        + [pltpu.VMEM((2, Z_DEV, depth, hidden), BF16)] + landing(hidden) + landing(hidden)
        + working(width) + landing(width, 2)
        + working(3 * width) + landing(3 * width)
        + [
            pltpu.VMEM((4, 16, D), F32), pltpu.VMEM((6, 16, D), F32),
            pltpu.SemaphoreType.DMA((copies,)), pltpu.SemaphoreType.DMA((copies,)),
            pltpu.SemaphoreType.DMA((6,)), pltpu.SemaphoreType.DMA((2, 2, 4)),
            pltpu.SemaphoreType.DMA((2, 7)),
            pltpu.VMEM((Z_DEV, depth // 2, 3 * width), BF16),
            pltpu.VMEM((3, depth // 2, 3 * width), BF16),
            pltpu.VMEM((2, depth // 2, 3 * width), BF16),
            pltpu.VMEM((3, Y_DEV, depth // 2, 3 * width), BF16),
            pltpu.VMEM((2, Y_DEV, depth // 2, 3 * width), BF16),
            pltpu.VMEM((Y_DEV, depth // 2, 3 * width), BF16),
            pltpu.VMEM((depth // 2, 3 * width), BF16),
        ],
        compiler_params=pltpu.CompilerParams(
            vmem_limit_bytes=VMEM_LIMIT, collective_id=2, has_side_effects=True
        ),
        name="fused_backward",
    )(tokens, gq, gw, rows, dh1, gb, gbt, q, v, kt, p, scale, o, a1t, layer, fold, work, early)


def place_gradients(
    tie_ref, sums_ref, part0_ref, partw_ref, part1_ref, part2_ref, near_out_ref,
    near_grad_ref, far_out_ref, far_grad_ref, gains_ref, bias_ref, in_ref, out_ref, expand_ref,
    project_ref, chosen_ref,
):
    t = pl.program_id(0)
    far_out_ref[...] = near_out_ref[...]
    far_grad_ref[...] = near_grad_ref[...]
    own = gains_ref.shape[-1]
    width = partw_ref.shape[-1]
    kinds = [tie_ref[0], tie_ref[1], tie_ref[2], tie_ref[3]]

    @pl.when(t == 0)
    def _():
        first = (lax.axis_index("dp") * 4 + lax.axis_index("tensor")) * own
        feature = lax.broadcasted_iota(jnp.int32, (D, 128), 0)
        lane = lax.broadcasted_iota(jnp.int32, (D, 128), 1)
        chosen = ((feature == first + lane) & (lane < own)).astype(F32)
        chosen_ref[...] = lax.dot_general(
            sums_ref[...], chosen, (((1,), (0,)), ((), ())),
            precision=lax.Precision.HIGHEST, preferred_element_type=F32,
        )
        row = lax.broadcasted_iota(jnp.int32, (NSRC, own), 0)
        for i, kind in enumerate([0, 0, 0, 1, 2, 3, 2, 2, 2, 2]):
            value = chosen_ref[2 + i : 3 + i, :own]
            bias_ref[i] = jnp.where(row == kinds[kind], value, 0.0)

    @pl.when(t < NSRC)
    def _():
        def here(kind, value):
            return jnp.where(kinds[kind] == t, value, jnp.zeros_like(value))

        gains_ref[0, 0:1] = here(0, chosen_ref[0:1, :own])
        gains_ref[0, 1:2] = here(2, chosen_ref[1:2, :own])
        for j in range(3):
            in_ref[0, j] = here(0, part0_ref[:, j * width : (j + 1) * width])
        out_ref[0] = here(1, partw_ref[...].T)
        expand_ref[0] = here(2, part1_ref[...])
        project_ref[0] = here(3, part2_ref[...])


def run_place_gradients(tie, sums, part0, partw, part1, part2, out, grad, like):
    slots, n, _ = grad.shape
    gains, biases, w_in, w_out, w_expand, w_project = [item.shape for item in like]
    shapes = [
        gains, (biases[1], biases[0], biases[2]), w_in, w_out, w_expand,
        (w_project[0], w_project[2], w_project[1]),
    ]

    def source(shape):
        return pl.BlockSpec(
            (1,) + shape[1:], lambda t: (jnp.minimum(t, NSRC - 1),) + (0,) * (len(shape) - 1)
        )

    half = pl.BlockSpec((1, n // 2, D), lambda t: (t // 2, t % 2, 0))
    out, grad, gains, biases, w_in, w_out, w_expand, w_project = pl.pallas_call(
        place_gradients,
        grid=(2 * slots,),
        in_specs=[SMEM_WHOLE] + [VMEM_WHOLE] * 5 + [half, half],
        out_specs=[half, half, source(shapes[0]), VMEM_WHOLE]
        + [source(shape) for shape in shapes[2:]],
        out_shape=[shaped(BF16, slots, n, D)] * 2 + [shaped(F32, *item) for item in shapes],
        scratch_shapes=[pltpu.VMEM((16, 128), F32)],
        compiler_params=pltpu.CompilerParams(vmem_limit_bytes=VMEM_LIMIT),
        name="place_gradients",
    )(tie, sums, part0, partw, part1, part2, out, grad)
    biases = biases.transpose(1, 0, 2)
    return out, grad, gains, biases, w_in, w_out, w_expand, w_project.transpose(0, 2, 1)


def plain_step(
    tokens, lengths, tie_map, norm_gains, bias_rows, attention_in, attention_out,
    expand_weight, project_weight, cotangent,
):
    slot_rows = tokens.shape[0] // lengths.shape[0]
    me = lax.axis_index("tensor")
    in_local = lax.dynamic_index_in_dim(attention_in, tie_map[0], 0, keepdims=False)
    out_local = lax.dynamic_index_in_dim(attention_out, tie_map[1], 0, keepdims=False)
    expand_local = lax.dynamic_index_in_dim(expand_weight, tie_map[2], 0, keepdims=False)
    project_local = lax.dynamic_index_in_dim(project_weight, tie_map[3], 0, keepdims=False)
    local0 = jnp.concatenate([in_local, out_local.T[None]], 0)
    row_kinds = jnp.array([0, 0, 0, 1, 2, 3] + [2] * (FF // D), dtype=jnp.int32)
    gain_kinds = jnp.array([0, 2], dtype=jnp.int32)
    gain_pick = norm_gains[tie_map[gain_kinds], jnp.arange(2)]
    bias_pick = bias_rows[tie_map[row_kinds], jnp.arange(row_kinds.shape[0])]
    vectors = jnp.concatenate([gain_pick, bias_pick], 0)
    x = lax.dynamic_slice_in_dim(tokens, me * slot_rows, slot_rows, 0)
    cot = lax.dynamic_slice_in_dim(cotangent, me * slot_rows, slot_rows, 0)
    length = lax.dynamic_slice_in_dim(lengths, me, 1, 0)
    rows = lax.all_gather(vectors, ("dp", "tensor"), axis=1, tiled=True).astype(F32)
    rows = jnp.concatenate([rows, jnp.zeros((4, D), F32)], 0)

    def gathered(piece, axis):
        piece = lax.all_gather(piece, "dp", axis=axis, tiled=True)
        return lax.all_gather(piece, "tensor", axis=0)

    g0 = gathered(local0, 1)
    g1 = gathered(expand_local, 0)
    g2 = gathered(project_local.T, 0)
    groups, width = g0.shape[0], g0.shape[-1]
    bqv = rows[3:5].reshape(2, groups, width).transpose(1, 0, 2)
    q, v, kt, p, o, a1t, h1, a2, a2t = run_attention_forward(length, x, g0, rows, bqv)
    out, d1, d2, dh1, gb, gbt, sums = run_feed_forward(length, cot, a2, a2t, h1, g1, g2, rows)
    d0, xg, sums_in, sums_qv = run_attention_backward(
        x, g0, rows, dh1, gb, gbt, q, v, kt, p, o, a1t
    )
    layer_out = lax.all_gather(out, "tensor", axis=0, tiled=True)
    tokens_grad = lax.all_gather(xg, "tensor", axis=0, tiled=True)

    def scattered(piece, axis):
        piece = lax.psum_scatter(piece, "tensor", scatter_dimension=0)
        return lax.psum_scatter(piece, "dp", scatter_dimension=axis, tiled=True).astype(F32)

    part0 = scattered(d0, 1)
    part1 = scattered(d1, 0)
    part2 = scattered(d2, 0)
    qv = sums_qv[:, :2].transpose(1, 0, 2).reshape(2, D)
    sums = jnp.concatenate(
        [sums_in[0:1], sums[1:2], sums_in[1:2], qv, sums[5:12]], 0
    )
    sums = lax.psum_scatter(sums, ("dp", "tensor"), scatter_dimension=1, tiled=True)
    return layer_out, tokens_grad, *placed(tie_map, sums, part0, part1, part2)


def fused_step(
    tokens, lengths, tie_map, norm_gains, bias_rows, attention_in, attention_out,
    expand_weight, project_weight, cotangent,
):
    slots = lengths.shape[0]
    tokens = tokens.reshape(slots, -1, D)
    cotangent = cotangent.reshape(slots, -1, D)
    gq, gw, g1, g2, rows, q, v, kt, p, scale, o, a1t, h1, a2, a2t = run_fused_forward(
        tie_map, lengths, tokens, norm_gains, bias_rows, attention_in, attention_out,
        expand_weight, project_weight,
    )
    layer, fold, work, dh1, gb, gbt, early = run_fused_feed_forward(
        lengths, cotangent, a2, a2t, h1, g1, g2, rows
    )
    grad, out, part0, partw, part1, part2, sums = run_fused_backward(
        tokens, gq, gw, rows, dh1, gb, gbt, q, v, kt, p, scale, o, a1t, layer, fold,
        work, early,
    )
    out, grad, *placed_grads = run_place_gradients(
        tie_map, sums, part0, partw, part1, part2, out, grad,
        (norm_gains, bias_rows, attention_in, attention_out, expand_weight, project_weight),
    )
    return out.reshape(-1, D), grad.reshape(-1, D), *placed_grads


def placed(tie_map, sums, part0, part1, part2):
    source = jnp.arange(NSRC, dtype=jnp.int32)

    def place(piece, which):
        pick = (source == tie_map[which]).reshape((NSRC,) + (1,) * piece.ndim)
        return jnp.where(pick, piece[None], 0.0)

    def place_rows(piece, kinds):
        pick = source[:, None] == tie_map[jnp.array(kinds, dtype=jnp.int32)][None, :]
        return jnp.where(pick[:, :, None], piece[None], 0.0)

    return (
        place_rows(sums[:2], [0, 2]),
        place_rows(sums[2:], [0, 0, 0, 1, 2, 3] + [2] * (FF // D)),
        place(part0[:3], 0),
        place(part0[3].T, 1),
        place(part1, 2),
        place(part2.T, 3),
    )


def solution(mesh):
    fused = mesh.shape["dp"] == Z_DEV * Y_DEV and mesh.shape["tensor"] == X_DEV * C_DEV
    return jax.shard_map(
        fused_step if fused else plain_step,
        mesh=mesh,
        in_specs=(
            P("dp", None),
            P("dp"),
            P(),
            P(None, None, ("dp", "tensor")),
            P(None, None, ("dp", "tensor")),
            P(None, None, "dp", "tensor"),
            P(None, "tensor", "dp"),
            P(None, "dp", "tensor"),
            P(None, "tensor", "dp"),
            P("dp", None),
        ),
        out_specs=(
            P("dp", None),
            P("dp", None),
            P(None, None, ("dp", "tensor")),
            P(None, None, ("dp", "tensor")),
            P(None, None, "dp", "tensor"),
            P(None, "tensor", "dp"),
            P(None, "dp", "tensor"),
            P(None, "tensor", "dp"),
        ),
        check_vma=False,
    )
```

```python
import jax
import jax.numpy as jnp
from jax import lax
from jax.experimental import pallas as pl
from jax.experimental.pallas import tpu as pltpu
from jax.sharding import PartitionSpec as P

D = 768
HEAD_DIM = 64
FF = 3072
NSRC = 4
EPS = 1e-05
MASKED = -1e30
F32 = jnp.float32
BF16 = jnp.bfloat16
VMEM_LIMIT = 60 * 1024 * 1024


def dot_nn(a, b):
    return lax.dot_general(a, b, (((1,), (0,)), ((), ())), preferred_element_type=F32)


def dot_nt(a, b):
    return lax.dot_general(a, b, (((1,), (1,)), ((), ())), preferred_element_type=F32)


def norm_parts(v):
    center = jnp.mean(v, -1, keepdims=True)
    centered = v - center
    r = lax.rsqrt(jnp.mean(centered * centered, -1, keepdims=True) + EPS)
    return centered * r, r


def head_mask(shape, h):
    lane = lax.broadcasted_iota(jnp.int32, shape, 1)
    return (lane >= h * HEAD_DIM) & (lane < (h + 1) * HEAD_DIM)


def blocks(total, size):
    return [slice(i * size, (i + 1) * size) for i in range(total // size)]


def attention_forward(
    len_ref, x_ref, g_ref, rows_ref, bqv_ref,
    q_ref, v_ref, kt_ref, p_ref, o_ref, a1t_ref, h1_ref, a2_ref, a2t_ref,
    a1_ref, k_ref, vt_ref, ot_ref, attn_ref,
):
    t = pl.program_id(0)
    n = x_ref.shape[0]
    width = g_ref.shape[-1]
    heads = width // HEAD_DIM
    step = 256
    length = len_ref[0]

    @pl.when(t == 0)
    def _():
        @pl.loop(0, n // step)
        def _(b):
            rows = pl.ds(pl.multiple_of(b * step, step), step)
            xhat, _ = norm_parts(x_ref[rows, :].astype(F32))
            a1 = xhat * rows_ref[0:1, :] + rows_ref[2:3, :]
            a1_ref[rows, :] = a1.astype(BF16)
            a1t_ref[:, rows] = a1.astype(BF16).T
            attn_ref[rows, :] = x_ref[rows, :].astype(F32) + rows_ref[5:6, :]

    @pl.loop(0, n // step)
    def _(b):
        rows = pl.ds(pl.multiple_of(b * step, step), step)
        a1 = a1_ref[rows, :]
        q = (dot_nn(a1, g_ref[0, 0]) + bqv_ref[0, 0:1, :]).astype(BF16)
        q_ref[0, rows, :] = q * jnp.asarray(HEAD_DIM ** -0.5, BF16)
        k = dot_nn(a1, g_ref[0, 1]).astype(BF16)
        k_ref[rows, :] = k
        kt_ref[0, :, rows] = k.T
        v = (dot_nn(a1, g_ref[0, 2]) + bqv_ref[0, 1:2, :]).astype(BF16)
        v_ref[0, rows, :] = v
        vt_ref[:, rows] = v.T

    for h in range(heads):
        k = k_ref[...]
        k = jnp.where(head_mask(k.shape, h), k, jnp.zeros_like(k))
        for b in range(n // step):
            first, last = b * step, (b + 1) * step
            q = q_ref[0, first:last, :]
            key = lax.broadcasted_iota(jnp.int32, (last, step), 0)
            query = lax.broadcasted_iota(jnp.int32, (step, step), 1) + first
            s = dot_nt(k[:last], q)
            near = jnp.where(
                (key[first:] <= query) & (key[first:] < length), s[first:], MASKED
            )
            if b:
                far = jnp.where(key[:first] < length, s[:first], MASKED)
                top = jnp.maximum(
                    jnp.max(far, 0, keepdims=True), jnp.max(near, 0, keepdims=True)
                )
                e_far = jnp.exp(far - top)
                e_near = jnp.exp(near - top)
                total = jnp.sum(e_far, 0, keepdims=True) + jnp.sum(e_near, 0, keepdims=True)
                scale = 1.0 / total
                p_ref[0, h, :first, first:last] = (e_far * scale).astype(BF16)
            else:
                top = jnp.max(near, 0, keepdims=True)
                e_near = jnp.exp(near - top)
                scale = 1.0 / jnp.sum(e_near, 0, keepdims=True)
            p_ref[0, h, first:last, first:last] = (e_near * scale).astype(BF16)
            ot_ref[h * HEAD_DIM : (h + 1) * HEAD_DIM, first:last] = dot_nn(
                vt_ref[h * HEAD_DIM : (h + 1) * HEAD_DIM, :last],
                p_ref[0, h, :last, first:last],
            ).astype(BF16)

    @pl.loop(0, n // step)
    def _(b):
        rows = pl.ds(pl.multiple_of(b * step, step), step)
        o = ot_ref[:, rows].T
        o_ref[0, rows, :] = o
        attn_ref[rows, :] += dot_nt(o, g_ref[0, 3])

    @pl.when(t == pl.num_programs(0) - 1)
    def _():
        @pl.loop(0, n // step)
        def _(b):
            rows = pl.ds(pl.multiple_of(b * step, step), step)
            h1 = attn_ref[rows, :]
            h1_ref[rows, :] = h1
            xhat, _ = norm_parts(h1)
            a2 = (xhat * rows_ref[1:2, :] + rows_ref[6:7, :]).astype(BF16)
            a2_ref[rows, :] = a2
            a2t_ref[:, rows] = a2.T


SQRT_2_PI = 0.7978845608028654


def feed_forward_both(
    len_ref, c_ref, a2_ref, a2t_ref, h1_ref, w1_ref, w2_ref, rows_ref,
    out_ref, d1_ref, d2_ref, dh1_ref, gb_ref, gbt_ref, sums_ref,
    gf_ref, gft_ref, feed_ref, da2_ref, h_ref, df_ref,
):
    t = pl.program_id(0)
    n = c_ref.shape[0]
    step = 256
    length = len_ref[0]

    @pl.when(t == 0)
    def _():
        sums_ref[...] = jnp.zeros_like(sums_ref)

        @pl.loop(0, n // step)
        def _(b):
            rows = pl.ds(pl.multiple_of(b * step, step), step)
            place = b * step + lax.broadcasted_iota(jnp.int32, (step, 1), 0)
            live = (place < length).astype(F32)
            g = (c_ref[rows, :].astype(F32) * live).astype(BF16)
            gf_ref[rows, :] = g
            gft_ref[:, rows] = g.T
            sums_ref[7:8, :] += jnp.sum(g.astype(F32), 0, keepdims=True)

    bias = rows_ref[pl.ds(8 + t, 1), :]

    @pl.loop(0, n // step)
    def _(b):
        rows = pl.ds(pl.multiple_of(b * step, step), step)
        f = dot_nn(a2_ref[rows, :], w1_ref[0]) + bias
        dh = dot_nn(gf_ref[rows, :], w2_ref[0])
        f2 = f * f
        th = jnp.tanh(f * (SQRT_2_PI + (SQRT_2_PI * 0.044715) * f2))
        half = 0.5 + 0.5 * th
        h = (f * half).astype(BF16)
        slope = half + f * (0.5 - 0.5 * th * th) * (
            SQRT_2_PI + (3 * SQRT_2_PI * 0.044715) * f2
        )
        df = (dh * slope).astype(BF16)
        h_ref[rows, :] = h
        df_ref[rows, :] = df
        sums_ref[pl.ds(8 + t, 1), :] += jnp.sum(df.astype(F32), 0, keepdims=True)
        feed = dot_nt(h, w2_ref[0])
        da2 = dot_nt(df, w1_ref[0])

        @pl.when(t == 0)
        def _():
            feed_ref[rows, :] = feed
            da2_ref[rows, :] = da2

        @pl.when(t > 0)
        def _():
            feed_ref[rows, :] += feed
            da2_ref[rows, :] += da2

    @pl.loop(0, D // step)
    def _(b):
        rows = pl.ds(pl.multiple_of(b * step, step), step)
        d1_ref[0, rows, :] = dot_nn(a2t_ref[rows, :], df_ref[...]).astype(BF16)
        d2_ref[0, rows, :] = dot_nn(gft_ref[rows, :], h_ref[...]).astype(BF16)

    @pl.when(t == pl.num_programs(0) - 1)
    def _():
        @pl.loop(0, n // step)
        def _(b):
            rows = pl.ds(pl.multiple_of(b * step, step), step)
            place = b * step + lax.broadcasted_iota(jnp.int32, (step, 1), 0)
            live = (place < length).astype(F32)
            h1 = h1_ref[rows, :]
            out_ref[rows, :] = (live * (h1 + (feed_ref[rows, :] + rows_ref[7:8, :]))).astype(BF16)
            xhat, r = norm_parts(h1)
            da2 = da2_ref[rows, :]
            sums_ref[1:2, :] += jnp.sum(da2 * xhat, 0, keepdims=True)
            sums_ref[6:7, :] += jnp.sum(da2, 0, keepdims=True)
            dg = da2 * rows_ref[1:2, :]
            dv = r * (
                dg
                - jnp.mean(dg, -1, keepdims=True)
                - xhat * jnp.mean(dg * xhat, -1, keepdims=True)
            )
            dh1 = live * c_ref[rows, :].astype(F32) + dv
            dh1_ref[rows, :] = dh1
            gb = dh1.astype(BF16)
            gb_ref[rows, :] = gb
            gbt_ref[:, rows] = gb.T
            sums_ref[5:6, :] += jnp.sum(gb.astype(F32), 0, keepdims=True)


def attention_backward(
    x_ref, g_ref, rows_ref, dh1_ref, gb_ref, gbt_ref, q_ref, v_ref, kt_ref, p_ref,
    o_ref, a1t_ref,
    d0_ref, xg_ref, sums_ref, bqv_ref,
    do_ref, delta_ref, dqt_ref, dq_ref, dk_ref, dv_ref, da1_ref,
):
    t = pl.program_id(0)
    n = x_ref.shape[0]
    width = g_ref.shape[-1]
    heads = width // HEAD_DIM
    step = 256
    pick = (
        lax.broadcasted_iota(jnp.int32, (16, width), 1) // HEAD_DIM
        == lax.broadcasted_iota(jnp.int32, (16, width), 0)
    ).astype(BF16)

    @pl.loop(0, n // step)
    def _(b):
        rows = pl.ds(pl.multiple_of(b * step, step), step)
        do = dot_nn(gb_ref[rows, :], g_ref[0, 3]).astype(BF16)
        do_ref[rows, :] = do
        prod = do.astype(F32) * o_ref[0, rows, :].astype(F32)
        high = prod.astype(BF16)
        low = (prod - high.astype(F32)).astype(BF16)
        delta_ref[:, rows] = dot_nt(pick, high) + dot_nt(pick, low)

    dqt_ref[...] = jnp.zeros_like(dqt_ref)
    for b in range(n // step):
        first, last = b * step, (b + 1) * step
        do = do_ref[first:, :]
        q = q_ref[0, first:, :]
        v = v_ref[0, first:last, :]
        dk, dv = None, None
        for h in range(heads):
            mine = head_mask((1, width), h)
            zero = jnp.zeros((), BF16)
            p = p_ref[0, h, first:last, first:]
            dp = dot_nt(jnp.where(mine, v, zero), do)
            ds = (p.astype(F32) * (dp - delta_ref[h : h + 1, first:])).astype(BF16)
            part = dot_nn(p, jnp.where(mine, do, zero))
            dv = part if dv is None else dv + part
            part = dot_nn(ds, jnp.where(mine, q, zero))
            dk = part if dk is None else dk + part
            head = slice(h * HEAD_DIM, (h + 1) * HEAD_DIM)
            dqt_ref[head, first:] += dot_nn(kt_ref[0, head, first:last], ds)
        dk_ref[first:last, :] = dk.astype(BF16)
        dv_ref[first:last, :] = dv.astype(BF16)

    @pl.when(t == 0)
    def _():
        da1_ref[...] = jnp.zeros_like(da1_ref)

    bqv_ref[...] = jnp.zeros_like(bqv_ref)

    @pl.loop(0, n // step)
    def _(b):
        rows = pl.ds(pl.multiple_of(b * step, step), step)
        dq = (dqt_ref[:, rows] * HEAD_DIM ** -0.5).astype(BF16).T
        dk = dk_ref[rows, :]
        dv = dv_ref[rows, :]
        dq_ref[rows, :] = dq
        bqv_ref[0, 0:1, :] += jnp.sum(dq.astype(F32), 0, keepdims=True)
        bqv_ref[0, 1:2, :] += jnp.sum(dv.astype(F32), 0, keepdims=True)
        da1_ref[rows, :] += (
            dot_nt(dq, g_ref[0, 0]) + dot_nt(dk, g_ref[0, 1]) + dot_nt(dv, g_ref[0, 2])
        )

    @pl.loop(0, D // step)
    def _(b):
        rows = pl.ds(pl.multiple_of(b * step, step), step)
        a1t = a1t_ref[rows, :]
        d0_ref[0, 0, rows, :] = dot_nn(a1t, dq_ref[...]).astype(BF16)
        d0_ref[0, 1, rows, :] = dot_nn(a1t, dk_ref[...]).astype(BF16)
        d0_ref[0, 2, rows, :] = dot_nn(a1t, dv_ref[...]).astype(BF16)
        d0_ref[0, 3, rows, :] = dot_nn(gbt_ref[rows, :], o_ref[0]).astype(BF16)

    @pl.when(t == pl.num_programs(0) - 1)
    def _():
        sums_ref[...] = jnp.zeros_like(sums_ref)

        @pl.loop(0, n // step)
        def _(b):
            rows = pl.ds(pl.multiple_of(b * step, step), step)
            xhat, r = norm_parts(x_ref[rows, :].astype(F32))
            da1 = da1_ref[rows, :]
            sums_ref[0:1, :] += jnp.sum(da1 * xhat, 0, keepdims=True)
            sums_ref[1:2, :] += jnp.sum(da1, 0, keepdims=True)
            dg = da1 * rows_ref[0:1, :]
            dv = r * (
                dg
                - jnp.mean(dg, -1, keepdims=True)
                - xhat * jnp.mean(dg * xhat, -1, keepdims=True)
            )
            xg_ref[rows, :] = (dh1_ref[rows, :] + dv).astype(BF16)


def whole(*shape):
    return pl.BlockSpec(shape, lambda t: (0,) * len(shape))


def group(*shape):
    return pl.BlockSpec((1,) + shape, lambda t: (t,) + (0,) * len(shape))


def shaped(dtype, *shape):
    return jax.ShapeDtypeStruct(shape, dtype)


SMEM_WHOLE = pl.BlockSpec(memory_space=pltpu.SMEM)


def run_attention_forward(length, x, g0, rows, bqv):
    n = x.shape[0]
    groups, _, _, width = g0.shape
    heads = width // HEAD_DIM
    return pl.pallas_call(
        attention_forward,
        grid=(groups,),
        in_specs=[SMEM_WHOLE, whole(n, D), group(4, D, width), whole(16, D), group(2, width)],
        out_specs=[
            group(n, width), group(n, width), group(width, n), group(heads, n, n),
            group(n, width), whole(D, n), whole(n, D), whole(n, D), whole(D, n),
        ],
        out_shape=[
            shaped(BF16, groups, n, width), shaped(BF16, groups, n, width),
            shaped(BF16, groups, width, n), shaped(BF16, groups, heads, n, n),
            shaped(BF16, groups, n, width), shaped(BF16, D, n), shaped(F32, n, D),
            shaped(BF16, n, D), shaped(BF16, D, n),
        ],
        scratch_shapes=[
            pltpu.VMEM((n, D), BF16), pltpu.VMEM((n, width), BF16),
            pltpu.VMEM((width, n), BF16), pltpu.VMEM((width, n), BF16),
            pltpu.VMEM((n, D), F32),
        ],
        compiler_params=pltpu.CompilerParams(vmem_limit_bytes=VMEM_LIMIT),
        name="attention_forward",
    )(length, x, g0, rows, bqv)


def run_feed_forward(length, cot, a2, a2t, h1, g1, g2, rows):
    n = cot.shape[0]
    groups, _, width = g1.shape
    return pl.pallas_call(
        feed_forward_both,
        grid=(groups,),
        in_specs=[
            SMEM_WHOLE, whole(n, D), whole(n, D), whole(D, n), whole(n, D),
            group(D, width), group(D, width), whole(16, D),
        ],
        out_specs=[
            whole(n, D), group(D, width), group(D, width), whole(n, D), whole(n, D),
            whole(D, n), whole(16, D),
        ],
        out_shape=[
            shaped(BF16, n, D), shaped(BF16, groups, D, width), shaped(BF16, groups, D, width),
            shaped(F32, n, D), shaped(BF16, n, D), shaped(BF16, D, n), shaped(F32, 16, D),
        ],
        scratch_shapes=[
            pltpu.VMEM((n, D), BF16), pltpu.VMEM((D, n), BF16), pltpu.VMEM((n, D), F32),
            pltpu.VMEM((n, D), F32), pltpu.VMEM((n, width), BF16), pltpu.VMEM((n, width), BF16),
        ],
        compiler_params=pltpu.CompilerParams(vmem_limit_bytes=VMEM_LIMIT),
        name="feed_forward_both",
    )(length, cot, a2, a2t, h1, g1, g2, rows)


def run_attention_backward(x, g0, rows, dh1, gb, gbt, q, v, kt, p, o, a1t):
    n = x.shape[0]
    groups, _, _, width = g0.shape
    heads = width // HEAD_DIM
    return pl.pallas_call(
        attention_backward,
        grid=(groups,),
        in_specs=[
            whole(n, D), group(4, D, width), whole(16, D), whole(n, D), whole(n, D),
            whole(D, n), group(n, width), group(n, width), group(width, n),
            group(heads, n, n), group(n, width), whole(D, n),
        ],
        out_specs=[group(4, D, width), whole(n, D), whole(8, D), group(8, width)],
        out_shape=[
            shaped(BF16, groups, 4, D, width), shaped(BF16, n, D), shaped(F32, 8, D),
            shaped(F32, groups, 8, width),
        ],
        scratch_shapes=[
            pltpu.VMEM((n, width), BF16), pltpu.VMEM((16, n), F32), pltpu.VMEM((width, n), F32),
            pltpu.VMEM((n, width), BF16), pltpu.VMEM((n, width), BF16),
            pltpu.VMEM((n, width), BF16), pltpu.VMEM((n, D), F32),
        ],
        compiler_params=pltpu.CompilerParams(vmem_limit_bytes=VMEM_LIMIT),
        name="attention_backward",
    )(x, g0, rows, dh1, gb, gbt, q, v, kt, p, o, a1t)


Z_DEV, Y_DEV, X_DEV, C_DEV = 4, 2, 2, 2


class Place:
    def __init__(self):
        dp, self.t = lax.axis_index("dp"), lax.axis_index("tensor")
        self.dp = dp
        self.z, self.y = dp // 2, dp % 2
        self.x, self.c = self.t // 2, self.t % 2
        self.other_y = 1 - self.y
        self.zs = [
            self.z,
            self.z + 1 - 2 * (self.z % 2),
            self.z + 2 - 4 * (self.z // 2),
            3 - self.z,
        ]
        self.ts = [
            self.t,
            self.t + 1 - 2 * (self.t % 2),
            self.t + 2 - 4 * (self.t // 2),
            3 - self.t,
        ]
        self.to_z = [dict(dp=z * 2 + self.y) for z in self.zs]
        self.to_y = dict(dp=self.z * 2 + self.other_y)
        self.to_x = dict(tensor=self.ts[2])
        self.same_t = self.to_z[1:] + [dict(dp=z * 2 + self.other_y) for z in self.zs]
        self.same_dp = [dict(tensor=t) for t in self.ts[1:]]
        self.to_core = dict(tensor=self.ts[1])

    def group(self, k):
        return lax.select(
            k == 0, self.ts[0],
            lax.select(k == 1, self.ts[1], lax.select(k == 2, self.ts[2], self.ts[3])),
        )

    def greet(self, others=None):
        barrier = pltpu.get_barrier_semaphore()
        others = others or self.to_z[1:] + [self.to_y, self.to_x, self.to_core]
        for device in others:
            pl.semaphore_signal(
                barrier, inc=1, device_id=device, device_id_type=pl.DeviceIdType.MESH
            )
        pl.semaphore_wait(barrier, len(others))


class Links:
    def __init__(self, send_sem, recv_sem):
        self.send_sem, self.recv_sem = send_sem, recv_sem
        self.copies = []

    def add(self, device, src, dst):
        number = len(self.copies)
        copy = pltpu.make_async_remote_copy(
            src_ref=src,
            dst_ref=dst,
            send_sem=self.send_sem.at[number],
            recv_sem=self.recv_sem.at[number],
            device_id=device,
            device_id_type=pl.DeviceIdType.MESH,
        )
        self.copies.append(copy)
        return copy

    def sent(self, *apart):
        for copy in self.copies:
            if all(copy is not other for other in apart):
                copy.wait_send()


def flat(copies):
    for item in copies:
        if isinstance(item, list):
            yield from flat(item)
        else:
            yield item


def start(*copies):
    for copy in flat(copies):
        copy.start()


def recv(*copies):
    for copy in flat(copies):
        copy.wait_recv()


class Gather:
    def __init__(self, links, place, own, full, order, single=True, last=True):
        every = slice(None)
        y, other = place.y, place.other_y

        def same(device, k, yy, to):
            return links.add(device, full(k, every, yy), full(to, every, yy))

        def along_z(k, yy, block):
            here, passed = full(k, place.z, yy), full(k, place.zs[2], yy)
            return [
                links.add(place.to_z[1], block, here),
                links.add(place.to_z[2], block, here),
                links.add(place.to_z[1], passed, passed),
            ]

        self.z = along_z(0, y, own)
        if order == X_Z_Y:
            self.first = [links.add(place.to_x, own, full(2, place.z, y))]
            self.far = along_z(2, y, full(2, place.z, y))
            blocks = [(0, y), (2, y), (0, other), (2, other)]
        else:
            blocks = [(0, y), (0, other), (2, y), (2, other)]
        if order == Y_Z_X:
            self.first = [links.add(place.to_y, own, full(0, place.z, y))]
            self.far = along_z(0, other, full(0, place.z, other))
        if order == Z_Y_X and single:
            self.first = [same(place.to_y, 0, y, 0)]
        if order == Z_Y_X and not single:
            self.first = [links.add(place.to_y, own, full(0, place.z, y))]
            for k in range(1, 4):
                block = full(0, place.zs[k], y)
                self.first.append(links.add(place.to_y, block, block))
        self.second = [
            same(place.to_y, k, yy, k) if order == X_Z_Y else same(place.to_x, k, yy, 2)
            for k, yy in blocks[: 2 if last else 1]
        ]
        if not last:
            blocks = [block for block in blocks if block[0] == 0]
        self.core = [same(place.to_core, k, yy, k + 1) for k, yy in blocks]


Z_Y_X, Y_Z_X, X_Z_Y = range(3)


def fused_forward(
    tie_ref, len_ref, tokens_ref, gains_ref, bias_ref, in_ref, out_ref, expand_ref,
    project_ref,
    gq_ref, gw_ref, flat1_ref, flat2_ref, rows_ref,
    q_ref, v_ref, kt_ref, p_ref, scale_ref, o_ref, a1t_out, h1_out, a2_out, a2t_out,
    own0_ref, ownw_ref, own1_ref, own2_ref, square_ref, vec_ref,
    all0_ref, allw_ref, w1_ref, w2_ref, vecs_ref, bqv_ref, x_ref, a1_ref, k_ref, qa_ref, vt_ref, ot_ref, a1t_ref, h1_ref, a2_ref, a2t_ref,
    send_sem, recv_sem, local_sem, flush_sem, row_sem,
):
    t = pl.program_id(0)
    n, _ = x_ref.shape
    width = allw_ref.shape[-1]
    heads = width // HEAD_DIM
    step = 256
    place = Place()
    length = len_ref[place.t]
    links = Links(send_sem, recv_sem)
    z, y, x, c = place.z, place.y, place.x, place.c
    mine_there = vecs_ref.at[z, y, x, c]
    column = vecs_ref.at[:, :, x, c]
    vec_one = [links.add(device, vec_ref, mine_there) for device in place.same_t]
    vec_two = [links.add(device, column, column) for device in place.same_dp]
    seg0 = Gather(
        links, place, own0_ref, lambda k, z, y: all0_ref.at[k, z, y], Z_Y_X, single=False
    )
    segw = Gather(links, place, ownw_ref, lambda k, z, y: allw_ref.at[k, z, y], Z_Y_X)
    seg1 = Gather(
        links, place, own1_ref, lambda k, z, y: w1_ref.at[k, z, y], Y_Z_X, last=False
    )
    seg2 = Gather(
        links, place, own2_ref, lambda k, z, y: w2_ref.at[k, z, y], X_Z_Y, last=False
    )
    flush = [
        [
            pltpu.make_async_copy(ref.at[k], flat.at[k], flush_sem.at[i, k])
            for k in range(3)
        ]
        for i, (ref, flat) in enumerate([(w1_ref, flat1_ref), (w2_ref, flat2_ref)])
    ]
    put_a1t = pltpu.make_async_copy(a1t_ref, a1t_out, local_sem.at[0])
    put_a2t = pltpu.make_async_copy(a2t_ref, a2t_out, local_sem.at[1])
    puts = []
    for i in range(n // step):
        rows = pl.ds(i * step, step)
        puts.append([
            pltpu.make_async_copy(h1_ref.at[rows], h1_out.at[rows], row_sem.at[0, i]),
            pltpu.make_async_copy(a2_ref.at[rows], a2_out.at[rows], row_sem.at[1, i]),
        ])
    fetch = pltpu.make_async_copy(tokens_ref.at[place.t], x_ref, local_sem.at[2])

    def relay_z(copies):
        recv(copies[1])
        start(copies[2])

    def pass_own(seg):
        recv(seg.z[0], seg.z[2])
        if seg is segw:
            start(seg.first)
        start(seg.second[0], seg.core[0])

    def pass_second(seg):
        recv(seg.second)
        if seg is seg2:
            start(seg.core[1])

    def pass_first(seg):
        recv(seg.first)
        if seg is segw:
            start(seg.second[1], seg.core[1])
        else:
            start(seg.far[1], seg.far[0])

    def pass_far(seg):
        recv(seg.far[0], seg.far[2])
        start(seg.core[1:] if seg is seg1 else [])

    def pass_core(seg, i):
        recv(seg.second[i])
        start(seg.core[2 + i])

    plan = [
        (0, 0, lambda: (pass_own(segw), pass_first(seg1), relay_z(seg2.z), pass_first(seg2))),
        (0, 2, lambda: (pass_first(segw), relay_z(seg1.z), pass_core(seg0, 0))),
        (1, 0, lambda: recv(seg0.core[:2])),
        (1, 1, lambda: relay_z(seg1.far)),
        (1, 2, lambda: (
            pass_core(seg0, 1), recv(segw.core[:2]), pass_core(segw, 0), pass_own(seg2),
        )),
        (2, 1, lambda: relay_z(seg2.far)),
        (2, 2, lambda: (pass_core(segw, 1), pass_own(seg1))),
        (3, 0, lambda: (recv(seg0.core[2:]), pass_far(seg1), flush[0][0].start())),
        (3, 1, lambda: (pass_second(seg2), flush[1][0].start())),
        (3, 2, lambda: (pass_far(seg2), flush[1][2].start(), recv(segw.core[2:]))),
    ]

    def serve(point):
        for step, where, act in plan:
            if where == point:
                pl.when(t == step)(lambda act=act: (act(), None)[1])

    @pl.when(t == 0)
    def _():
        s0, s1, s2, s3 = tie_ref[0], tie_ref[1], tie_ref[2], tie_ref[3]
        fetch.start()
        square_ref[...] = jnp.zeros_like(square_ref)
        gain = gains_ref.shape[-1]
        square_ref[0:1, :gain] = gains_ref[s0].astype(F32)[0:1]
        square_ref[1:2, :gain] = gains_ref[s2].astype(F32)[1:2]
        kinds = [s0, s0, s0, s1, s2, s3, s2, s2, s2, s2]
        for i, source in enumerate(kinds):
            wide = bias_ref[i].astype(F32)
            here = lax.broadcasted_iota(jnp.int32, wide.shape, 0) == source
            square_ref[2 + i : 3 + i, :gain] = jnp.sum(
                jnp.where(here, wide, 0.0), 0, keepdims=True
            )
        vec_ref[...] = square_ref[...].T[:gain]
        for j in range(3):
            own0_ref[:, j * width : (j + 1) * width] = in_ref[s0, j]
        place.greet(place.same_t + place.same_dp)
        start(vec_one, seg0.z[1], seg0.z[0], seg0.first[0])
        vecs_ref[z, y, x, c] = vec_ref[...]
        ones = lax.broadcasted_iota(jnp.int32, (vt_ref.shape[1] - HEAD_DIM, n), 0) == 0
        for h in range(heads):
            vt_ref[h, HEAD_DIM:, :] = ones.astype(BF16)
        all0_ref[0, z, y] = own0_ref[...]
        ownw_ref[...] = out_ref[s1].T
        allw_ref[0, z, y] = ownw_ref[...]
        own1_ref[...] = expand_ref[s2]
        own2_ref[...] = project_ref[s3]
        w1_ref[0, z, y] = own1_ref[...]
        w2_ref[0, z, y] = own2_ref[...]
        recv(vec_one)
        start(vec_two)
        relay_z(seg0.z)
        start(seg0.first[2])
        recv(seg0.z[0])
        start(seg0.first[1], segw.z[1], segw.z[0], seg2.z[1])
        recv(vec_two)
        start(seg2.first)
        vecs = vecs_ref[...].reshape(D, vecs_ref.shape[-1]).T[:16]
        rows_ref[...] = vecs
        recv(seg0.z[2])
        start(seg0.first[3], seg1.first, seg0.second[0], seg0.core[0])
        for k in range(4):
            part = slice(k * width, (k + 1) * width)
            bqv_ref[k, 0:1, :width] = vecs[3:4, part]
            bqv_ref[k, 0:1, width : 2 * width] = jnp.zeros((1, width), F32)
            bqv_ref[k, 0:1, 2 * width :] = vecs[4:5, part]
        fetch.wait()

        @pl.loop(0, n // step)
        def _(b):
            rows = pl.ds(pl.multiple_of(b * step, step), step)
            wide = x_ref[rows, :].astype(F32)
            xhat, _ = norm_parts(wide)
            a1 = (xhat * rows_ref[0:1, :] + rows_ref[2:3, :]).astype(BF16)
            a1_ref[rows, :] = a1
            a1t_ref[:, rows] = a1.T
            h1_ref[rows, :] = wide + rows_ref[5:6, :]

        put_a1t.start()
        relay_z(segw.z)
        start(seg2.z[0], seg1.z[1], seg1.z[0])
        recv(seg0.first)
        start(seg0.second[1], seg0.core[1])

    serve(0)
    gq = all0_ref[t].reshape(D, 3 * width)
    gq_ref[0] = gq
    mine = place.group(t)
    qkv = dot_nn(a1_ref[...], gq) + bqv_ref[mine, 0:1, :]
    q = qkv[:, :width].astype(BF16) * jnp.asarray(HEAD_DIM ** -0.5, BF16)
    k = qkv[:, width : 2 * width].astype(BF16)
    v = qkv[:, 2 * width :].astype(BF16)
    q_ref[0] = q
    kt_ref[0] = k.T
    v_ref[0] = v
    vt = v.T
    for h in range(heads):
        vt_ref[h, :HEAD_DIM, :] = vt[h * HEAD_DIM : (h + 1) * HEAD_DIM]
    spare = k_ref.shape[1] - width
    dead = lax.broadcasted_iota(jnp.int32, (n, spare), 0) >= length
    first_column = lax.broadcasted_iota(jnp.int32, (n, spare), 1) == 0
    k_ref[:, :width] = k
    k_ref[:, width:] = jnp.where(first_column & dead, MASKED, 0.0).astype(BF16)
    qa_ref[:, :width] = q
    qa_ref[:, width:] = jnp.where(first_column, 1.0, 0.0).astype(BF16)

    serve(1)
    def scores(h, b):
        first, last = b * step, (b + 1) * step
        q = qa_ref[first:last, :]
        lane = lax.broadcasted_iota(jnp.int32, (1, q.shape[1]), 1)
        keep = head_mask((1, q.shape[1]), h) | (lane >= width)
        return dot_nt(k_ref[:last, :], jnp.where(keep, q, jnp.zeros((), BF16)))

    def attend(h, b, s):
        first, last = b * step, (b + 1) * step
        key = lax.broadcasted_iota(jnp.int32, (step, step), 0)
        query = lax.broadcasted_iota(jnp.int32, (step, step), 1)
        near = jnp.where(key <= query, s[first:], MASKED)
        top = jnp.max(near, 0, keepdims=True)
        if b:
            far = s[:first]
            top = jnp.maximum(top, jnp.max(far, 0, keepdims=True))
        e_near = jnp.exp((near - top).astype(BF16))
        p_ref[0, h, b, first:last, :] = e_near
        o = dot_nn(vt_ref[h, :, first:last], e_near)
        if b:
            e_far = jnp.exp((far - top).astype(BF16))
            p_ref[0, h, b, :first, :] = e_far
            o += dot_nn(vt_ref[h, :, :first], e_far)
        scale = 1.0 / o[HEAD_DIM : HEAD_DIM + 1]
        scale_ref[0, h : h + 1, first:last] = scale
        ot_ref[h * HEAD_DIM : (h + 1) * HEAD_DIM, first:last] = (
            o[:HEAD_DIM] * scale
        ).astype(BF16)

    scale_ref[0, heads:, :] = jnp.zeros((scale_ref.shape[1] - heads, n), F32)
    ready = [scores(h, 0) for h in range(heads)]
    for b in range(n // step):
        ahead = [scores(h, b + 1) for h in range(heads)] if b + 1 < n // step else None
        for h in range(heads):
            attend(h, b, ready[h])
        ready = ahead
    serve(2)

    gw_ref[0] = allw_ref[t].reshape(gw_ref.shape[1:])
    o = ot_ref[...].T
    o_ref[0] = o
    h1_ref[...] += dot_nt(o, gw_ref[0])

    @pl.when(t == 3)
    def _():
        for i, rows in enumerate(blocks(n, step)):
            xhat, _ = norm_parts(h1_ref[rows, :])
            a2 = (xhat * rows_ref[1:2, :] + rows_ref[6:7, :]).astype(BF16)
            a2_ref[rows, :] = a2
            a2t_ref[:, rows] = a2.T
            for put in puts[i]:
                put.start()
        put_a2t.start()
        recv(seg2.core)
        flush[1][1].start()
        recv(seg1.core)
        flush[0][1].start()
        pass_second(seg1)
        flush[0][2].start()
        links.sent()
        for copies in flush + puts + [[put_a1t, put_a2t]]:
            for copy in copies:
                copy.wait()


N_GATHER = 10 + 13 + 10 + 10 + 10
VMEM_WHOLE = pl.BlockSpec(memory_space=pltpu.VMEM)
ANY_WHOLE = pl.BlockSpec(memory_space=pl.ANY)


def run_fused_forward(tie, lengths, tokens, gains, biases, w_in, w_out, w_expand, w_project):
    groups, n, _ = tokens.shape
    depth, width = w_in.shape[-2:]
    heads = width // HEAD_DIM
    hidden = w_expand.shape[-1]
    w_project = w_project.transpose(0, 2, 1)
    biases = biases.transpose(1, 0, 2)
    own = gains.shape[-1]
    return pl.pallas_call(
        fused_forward,
        grid=(groups,),
        in_specs=[SMEM_WHOLE, SMEM_WHOLE, ANY_WHOLE] + [VMEM_WHOLE] * 6,
        out_specs=[
            group(D, 3 * width), group(D, width), ANY_WHOLE, ANY_WHOLE, VMEM_WHOLE,
            group(n, width), group(n, width), group(width, n), group(heads, n // 256, n, 256),
            group(8, n), group(n, width), ANY_WHOLE, ANY_WHOLE, ANY_WHOLE, ANY_WHOLE,
        ],
        out_shape=[
            shaped(BF16, groups, D, 3 * width), shaped(BF16, groups, D, width),
            shaped(BF16, groups, Z_DEV, Y_DEV, depth, hidden),
            shaped(BF16, groups, Z_DEV, Y_DEV, depth, hidden),
            shaped(F32, 16, D),
            shaped(BF16, groups, n, width), shaped(BF16, groups, n, width),
            shaped(BF16, groups, width, n), shaped(BF16, groups, heads, n // 256, n, 256),
            shaped(F32, groups, 8, n), shaped(BF16, groups, n, width), shaped(BF16, D, n), shaped(F32, n, D),
            shaped(BF16, n, D), shaped(BF16, D, n),
        ],
        scratch_shapes=[
            pltpu.VMEM((depth, 3 * width), BF16), pltpu.VMEM((depth, width), BF16),
            pltpu.VMEM((depth, hidden), BF16), pltpu.VMEM((depth, hidden), BF16),
            pltpu.VMEM((128, 128), F32), pltpu.VMEM((own, 128), F32),
            pltpu.VMEM((groups, Z_DEV, Y_DEV, depth, 3 * width), BF16),
            pltpu.VMEM((groups, Z_DEV, Y_DEV, depth, width), BF16),
            pltpu.VMEM((groups, Z_DEV, Y_DEV, depth, hidden), BF16),
            pltpu.VMEM((groups, Z_DEV, Y_DEV, depth, hidden), BF16),
            pltpu.VMEM((Z_DEV, Y_DEV, X_DEV, C_DEV, own, 128), F32),
            pltpu.VMEM((groups, 8, 3 * width), F32),
            pltpu.VMEM((n, D), BF16), pltpu.VMEM((n, D), BF16), pltpu.VMEM((n, 256), BF16),
            pltpu.VMEM((n, 256), BF16), pltpu.VMEM((heads, HEAD_DIM + 16, n), BF16),
            pltpu.VMEM((width, n), BF16),
            pltpu.VMEM((D, n), BF16), pltpu.VMEM((n, D), F32), pltpu.VMEM((n, D), BF16),
            pltpu.VMEM((D, n), BF16),
            pltpu.SemaphoreType.DMA((N_GATHER,)), pltpu.SemaphoreType.DMA((N_GATHER,)),
            pltpu.SemaphoreType.DMA((3,)), pltpu.SemaphoreType.DMA((2, 4)),
            pltpu.SemaphoreType.DMA((2, n // 256)),
        ],
        compiler_params=pltpu.CompilerParams(
            vmem_limit_bytes=VMEM_LIMIT, collective_id=0, has_side_effects=True
        ),
        name="fused_forward",
    )(tie, lengths, tokens, gains, biases, w_in, w_out, w_expand, w_project)


class Result:
    def __init__(self, links, place, own_ref, passing_ref, out_ref, step, sem, count):
        self.x, self.core, self.far, self.keep, self.keep_far = [], [], [], [], []
        for i in range(count):
            rows = pl.ds(i * step, step)
            mine, theirs = out_ref.at[place.t, rows], out_ref.at[place.ts[2], rows]
            own, passing = own_ref.at[rows], passing_ref.at[rows]
            self.x.append(links.add(place.to_x, own, passing))
            self.core.append(links.add(place.to_core, own, mine))
            self.far.append(links.add(place.to_core, passing, theirs))
            self.keep.append(pltpu.make_async_copy(own, mine, sem.at[0, i]))
            self.keep_far.append(pltpu.make_async_copy(passing, theirs, sem.at[1, i]))

    def send(self, i):
        start(self.x[i], self.core[i], self.keep[i])

    def pass_on(self, i):
        recv(self.x[i])
        start(self.far[i], self.keep_far[i])

    def finish(self):
        recv(self.core, self.far)
        for copy in self.keep + self.keep_far:
            copy.wait()


def low(value):
    return jnp.asarray(value, BF16)


def pair_order(i):
    return i + 1 - 2 * (i % 2)


def fused_feed_forward(
    len_ref, cot_ref, a2_ref, a2t_in, h1_in, far1_ref, far2_ref, rows_ref,
    out_out, fold_ref, work_out, dh1_out, gb_out, gbt_out, sums_ref,
    gf_ref, gft_ref, feed_ref, da2_ref, h_ref, df_ref, weights_ref, missing_ref, third_ref,
    stage_ref, land_ref, near_ref, cross_ref, a2t_ref, h1_ref, out_ref, work_ref,
    send_sem, recv_sem, local_sem, row_sem,
):
    t = pl.program_id(0)
    n = gf_ref.shape[0]
    step = 256
    depth = stage_ref.shape[-2]
    place = Place()
    length = len_ref[place.t]
    links = Links(send_sem, recv_sem)
    y, other = place.y, place.other_y
    last = [
        links.add(place.to_x, far1_ref.at[0, :, other], missing_ref.at[0, 0]),
        links.add(place.to_y, far2_ref.at[2, :, y], missing_ref.at[1, 0]),
    ]
    last_core = [
        links.add(place.to_core, missing_ref.at[i, 0], missing_ref.at[i, 1]) for i in range(2)
    ]
    third = [
        links.add(place.to_core, far_ref.at[2, :, y], third_ref.at[i])
        for i, far_ref in enumerate([far1_ref, far2_ref])
    ]
    core = [
        [links.add(place.to_core, stage_ref.at[i], land_ref.at[s, i]) for i in range(2)]
        for s in range(2)
    ]
    cross = [
        links.add(place.to_y, near_ref.at[i, :, other], cross_ref.at[i]) for i in range(2)
    ]
    fetch = pltpu.make_async_copy(cot_ref.at[place.t], gf_ref, local_sem.at[0])
    gb_ref, gbt_ref, dh1_ref = gf_ref, gft_ref, da2_ref
    late = [
        pltpu.make_async_copy(a2t_in, a2t_ref, local_sem.at[5]),
        pltpu.make_async_copy(h1_in, h1_ref, local_sem.at[6]),
    ]
    puts = []
    for i in range(n // step):
        rows = pl.ds(i * step, step)
        puts.append([
            pltpu.make_async_copy(ref.at[rows], out.at[rows], row_sem.at[j, i])
            for j, (ref, out) in enumerate(
                [(out_ref, out_out), (dh1_ref, dh1_out), (gb_ref, gb_out)]
            )
        ])
    put_gbt = pltpu.make_async_copy(gbt_ref, gbt_out, local_sem.at[7])
    put_work = pltpu.make_async_copy(work_ref, work_out, local_sem.at[8])
    k = pair_order(t)
    mine = place.group(k)

    def load(step, whole, slot):
        for i, far_ref in enumerate([far1_ref, far2_ref]):
            group = far_ref.at[pair_order(step)]
            to = weights_ref.at[slot, i]
            if not whole:
                group, to = group.at[:, y], to.at[:, y]
            yield pltpu.make_async_copy(group, to, local_sem.at[1 + 2 * slot + i])

    def live_rows(b):
        at = b * step + lax.broadcasted_iota(jnp.int32, (step, 1), 0)
        return (at < length).astype(F32)

    @pl.when(t == 0)
    def _():
        fetch.start()
        for copy in load(0, True, 0):
            copy.start()
        for copy in late:
            copy.start()
        place.greet()
        start(last, third)
        sums_ref[...] = jnp.zeros_like(sums_ref)
        feed_ref[...] = jnp.zeros_like(feed_ref)
        da2_ref[...] = jnp.zeros_like(da2_ref)
        fetch.wait()

        @pl.loop(0, n // step)
        def _(b):
            rows = pl.ds(pl.multiple_of(b * step, step), step)
            g = (gf_ref[rows, :].astype(F32) * live_rows(b)).astype(BF16)
            gf_ref[rows, :] = g
            gft_ref[:, rows] = g.T
            sums_ref[7:8, :] += jnp.sum(g.astype(F32), 0, keepdims=True)

    for i in range(4):
        @pl.when(t == i)
        def _():
            if i == 2:
                recv(last_core, third)
            else:
                for copy in load(i, i < 2, i % 2):
                    copy.wait()
            if i in (0, 2):
                for copy in load(i + 1, i + 1 < 2, (i + 1) % 2):
                    copy.start()
            for j in range(2):
                if i == 2:
                    weights_ref[0, j, :, y] = third_ref[j]
                if i >= 2:
                    weights_ref[i % 2, j, :, other] = missing_ref[j, 3 - i]

    bias = rows_ref[pl.ds(8 + mine, 1), :]
    w1 = weights_ref[t % 2, 0].reshape(D, -1)
    w2 = weights_ref[t % 2, 1].reshape(D, -1)
    column = jnp.zeros((1, w1.shape[1]), F32)
    for rows in blocks(n, step):
        f = (dot_nn(a2_ref[rows, :], w1) + bias).astype(BF16)
        dh = dot_nn(gf_ref[rows, :], w2)
        f2 = f * f
        th = jnp.tanh(f * (low(SQRT_2_PI) + low(SQRT_2_PI * 0.044715) * f2))
        half = low(0.5) + low(0.5) * th
        h = f * half
        slope = half + f * (low(0.5) - low(0.5) * th * th) * (
            low(SQRT_2_PI) + low(3 * SQRT_2_PI * 0.044715) * f2
        )
        df = (dh * slope.astype(F32)).astype(BF16)
        h_ref[rows, :] = h
        df_ref[rows, :] = df
        column += jnp.sum(df.astype(F32), 0, keepdims=True)
        feed_ref[rows, :] += dot_nt(h, w2)
        da2_ref[rows, :] += dot_nt(df, w1)
    sums_ref[pl.ds(8 + mine, 1), :] = column

    @pl.when(t == 1)
    def _():
        recv(last)
        start(last_core)

    @pl.when(t == 0)
    def _():
        late[0].wait()

    def weight_grad(left_ref, right_ref):
        value = dot_nn(left_ref[...], right_ref[...])
        return value.reshape(Z_DEV, Y_DEV, depth, value.shape[-1]).astype(BF16)

    grad1 = weight_grad(a2t_ref, df_ref)
    grad2 = weight_grad(gft_ref, h_ref)

    def put(ref):
        ref[0] = grad1
        ref[1] = grad2

    def reduced(ref):
        return lambda i, s, z: (
            ref[i, z].astype(F32) + land_ref[s, i, z].astype(F32)
        ).astype(BF16)

    @pl.when(t == 0)
    def _():
        put(stage_ref)
        start(core[0])

    @pl.when(t == 1)
    def _():
        put(near_ref)
        recv(core[0])

        @pl.loop(0, Z_DEV)
        def _(z):
            for i in range(2):
                near_ref[i, z] = reduced(near_ref)(i, 0, z)

        start(cross)

    @pl.when(t == 2)
    def _():
        for copy in core[0]:
            copy.wait_send()
        put(stage_ref)
        start(core[1])

    @pl.when(t == 3)
    def _():
        put(work_ref)
        late[1].wait()
        for i, rows in enumerate(blocks(n, step)):
            live = live_rows(i)
            h1 = h1_ref[rows, :]
            out_ref[rows, :] = (live * (h1 + (feed_ref[rows, :] + rows_ref[7:8, :]))).astype(BF16)
            xhat, r = norm_parts(h1)
            da2 = da2_ref[rows, :]
            sums_ref[1:2, :] += jnp.sum(da2 * xhat, 0, keepdims=True)
            sums_ref[6:7, :] += jnp.sum(da2, 0, keepdims=True)
            dg = da2 * rows_ref[1:2, :]
            dv = r * (
                dg
                - jnp.mean(dg, -1, keepdims=True)
                - xhat * jnp.mean(dg * xhat, -1, keepdims=True)
            )
            dh1 = gf_ref[rows, :].astype(F32) + dv
            dh1_ref[rows, :] = dh1
            gb = dh1.astype(BF16)
            gb_ref[rows, :] = gb
            gbt_ref[:, rows] = gb.T
            sums_ref[5:6, :] += jnp.sum(gb.astype(F32), 0, keepdims=True)
            for copy in puts[i]:
                copy.start()
        put_gbt.start()
        recv(core[1])

        @pl.loop(0, Z_DEV)
        def _(z):
            for i in range(2):
                work_ref[i, z] = reduced(work_ref)(i, 1, z)

        put_work.start()
        recv(cross)

        @pl.loop(0, Z_DEV)
        def _(z):
            for i in range(2):
                fold_ref[i, z] = (
                    near_ref[i, z, y].astype(F32) + cross_ref[i, z].astype(F32)
                ).astype(BF16)

        links.sent(*core[0])
        for copies in puts + [[put_gbt, put_work]]:
            for copy in copies:
                copy.wait()


def run_fused_feed_forward(lengths, cot, a2, a2t, h1, g1, g2, rows):
    n = cot.shape[1]
    groups, _, _, depth, hidden = g1.shape
    both = (2, Z_DEV, Y_DEV, depth, hidden)
    fold = (2, Z_DEV, depth, hidden)
    return pl.pallas_call(
        fused_feed_forward,
        grid=(groups,),
        in_specs=[SMEM_WHOLE, ANY_WHOLE, VMEM_WHOLE] + [ANY_WHOLE] * 4 + [VMEM_WHOLE],
        out_specs=[ANY_WHOLE, VMEM_WHOLE] + [ANY_WHOLE] * 4 + [VMEM_WHOLE],
        out_shape=[
            shaped(BF16, n, D), shaped(BF16, *fold), shaped(BF16, *both), shaped(F32, n, D),
            shaped(BF16, n, D), shaped(BF16, D, n), shaped(F32, 16, D),
        ],
        scratch_shapes=[
            pltpu.VMEM((n, D), BF16), pltpu.VMEM((D, n), BF16), pltpu.VMEM((n, D), F32),
            pltpu.VMEM((n, D), F32), pltpu.VMEM((n, hidden), BF16), pltpu.VMEM((n, hidden), BF16),
            pltpu.VMEM((2,) + both, BF16),
            pltpu.VMEM((2,) + fold, BF16), pltpu.VMEM(fold, BF16), pltpu.VMEM(both, BF16),
            pltpu.VMEM((2,) + both, BF16),
            pltpu.VMEM(both, BF16), pltpu.VMEM(fold, BF16),
            pltpu.VMEM((D, n), BF16), pltpu.VMEM((n, D), F32), pltpu.VMEM((n, D), BF16),
            pltpu.VMEM(both, BF16),
            pltpu.SemaphoreType.DMA((12,)), pltpu.SemaphoreType.DMA((12,)),
            pltpu.SemaphoreType.DMA((9,)), pltpu.SemaphoreType.DMA((3, n // 256)),
        ],
        compiler_params=pltpu.CompilerParams(
            vmem_limit_bytes=VMEM_LIMIT, collective_id=1, has_side_effects=True
        ),
        name="fused_feed_forward",
    )(lengths, cot, a2, a2t, h1, g1, g2, rows)
class Reduce:
    def __init__(
        self, links, place, work, acc, cross_ref, far_ref, mid_ref, last_ref, side_ref,
        slots=(0, 1), split=False,
    ):
        self.place, self.work, self.acc = place, work, acc
        self.cross_ref, self.far_ref, self.mid_ref = cross_ref, far_ref, mid_ref
        self.last_ref, self.side_ref = last_ref, side_ref
        self.two = len(slots) == 2
        zs = place.zs
        self.y = {
            s: [
                links.add(
                    place.to_y, work(s, zs[j], place.other_y),
                    cross_ref.at[s if self.two else 0, zs[j]],
                )
                for j in (1, 3, 2, 0)
            ]
            for s in slots
        }
        self.z = [
            [
                links.add(place.to_z[1], acc(s, zs[1]), far_ref.at[s, 0]),
                links.add(place.to_z[1], acc(s, zs[3]), far_ref.at[s, 1]),
                links.add(place.to_z[2], mid_ref.at[s, 1], far_ref.at[s, 2]),
            ]
            for s in range(1 if split else 2)
        ]
        self.x = links.add(place.to_x, last_ref, side_ref)

    def fold_y(self, s, half):
        for i, j in [(0, 1), (1, 3), (2, 2), (3, 0)][2 * half : 2 * half + 2]:
            z = self.place.zs[j]
            recv(self.y[s][i])
            value = self.work(s, z, self.place.y)[...].astype(F32)
            cross = self.cross_ref[s if self.two else 0, z].astype(F32)
            self.acc(s, z)[...] = (value + cross).astype(BF16)
            if i < 2:
                start(self.z[s][i])

    def fold_z(self, s):
        recv(self.z[s][:2])
        for i in (1, 0):
            value = self.acc(s, self.place.zs[2 * i])[...].astype(F32)
            self.mid_ref[s, i] = (value + self.far_ref[s, i].astype(F32)).astype(BF16)
            if i:
                start(self.z[s][2])

    def own(self, s):
        recv(self.z[s][2])
        return self.mid_ref[s, 0].astype(F32) + self.far_ref[s, 2].astype(F32)

    def send_x(self):
        self.last_ref[...] = self.own(1).astype(BF16)
        start(self.x)

    def total(self):
        value = self.own(0)
        recv(self.x)
        return value + self.side_ref[...].astype(F32)


class ReduceHalves:
    def __init__(self, links, place, work, landings, last_ref):
        self.place, self.work = place, work
        self.cross, self.far, self.mid, self.far2, self.mid2, self.fin2, self.cross2 = landings
        self.last_ref = last_ref
        zs, half = place.zs, last_ref.shape[0] // 2
        self.low, self.high = pl.ds(0, half), pl.ds(half, half)
        every = slice(None)
        y, other = place.y, place.other_y
        self.y = [
            links.add(place.to_y, work.at[zs[j], other, self.low], self.cross.at[zs[j]])
            for j in (1, 3, 2, 0)
        ]
        self.z = [
            links.add(place.to_z[1], work.at[zs[1], y, self.low], self.far.at[0]),
            links.add(place.to_z[1], work.at[zs[3], y, self.low], self.far.at[1]),
            links.add(place.to_z[2], self.mid.at[1], self.far.at[2]),
        ]
        self.z2 = [
            links.add(place.to_z[1], work.at[zs[1], every, self.high], self.far2.at[0]),
            links.add(place.to_z[1], work.at[zs[3], every, self.high], self.far2.at[1]),
            links.add(place.to_z[2], self.mid2.at[1], self.far2.at[2]),
        ]
        self.y2 = links.add(place.to_y, self.fin2.at[other], self.cross2)

    def begin(self):
        start(self.y, self.z2[:2])

    def add(self, target, left, right):
        target[...] = (left[...].astype(F32) + right[...].astype(F32)).astype(BF16)

    def fold_y(self):
        y, zs = self.place.y, self.place.zs
        for i, j in enumerate((1, 3, 2, 0)):
            recv(self.y[i])
            block = self.work.at[zs[j], y, self.low]
            self.add(block, block, self.cross.at[zs[j]])
            if i < 2:
                start(self.z[i])

    def fold_high(self):
        recv(self.z2[:2])
        for i in (1, 0):
            block = self.work.at[self.place.zs[2 * i], :, self.high]
            self.add(self.mid2.at[i], block, self.far2.at[i])
            if i:
                start(self.z2[2])

    def cross_high(self):
        recv(self.z2[2])
        self.add(self.fin2, self.mid2.at[0], self.far2.at[2])
        start(self.y2)

    def fold_z(self):
        recv(self.z[:2])
        for i in (1, 0):
            block = self.work.at[self.place.zs[2 * i], self.place.y, self.low]
            self.add(self.mid.at[i], block, self.far.at[i])
            if i:
                start(self.z[2])

    def finish(self):
        recv(self.z[2])
        self.add(self.last_ref.at[self.low], self.mid.at[0], self.far.at[2])
        recv(self.y2)
        self.add(self.last_ref.at[self.high], self.fin2.at[self.place.y], self.cross2)


def fused_backward(
    tokens_ref, gq_in, gw_in, rows_ref, dh1_ref, gb_ref, gbt_in, q_in, v_in, kt_in,
    p_ref, scale_in, o_in, a1t_in, layer_in, fold_in, work_in, early_ref,
    out_ref, layerout_ref, part0_ref, partw_ref, part1_ref, part2_ref, total_ref,
    gq_ref, gw_ref, q_ref, v_ref, kt_ref, scale_ref, o_ref,
    a1t_ref, gbt_ref, layer_ref, fold_ref, work_ref, do_ref, delta_ref, dkv_ref, dqkv_ref, da1_ref, own_ref, passing_ref, passlayer_ref, bqv_ref,
    folded_ref, cross1_ref, far1_ref, mid1_ref, last1_ref, side1_ref,
    cross2_ref, far2_ref, mid2_ref, last2_ref, side2_ref,
    stagew_ref, landw_ref, workw_ref, crossw_ref, farw_ref, midw_ref, lastw_ref, sidew_ref,
    stage0_ref, land0_ref, work0_ref, cross0_ref, far0_ref, mid0_ref, last0_ref, side0_ref,
    sums_ref, sumland_ref,
    send_sem, recv_sem, local_sem, result_sem, group_sem, *tail_refs,
):
    t = pl.program_id(0)
    n = own_ref.shape[0]
    width = gw_ref.shape[-1]
    depth = part0_ref.shape[0]
    heads = width // HEAD_DIM
    step = n // 4
    place = Place()
    y = place.y
    links = Links(send_sem, recv_sem)
    k, i = group_and_block(t)
    mine = place.group(k)
    now = k % 2
    out = Result(links, place, own_ref, passing_ref, out_ref, step, result_sem.at[0], 4)
    layer = Result(links, place, layer_ref, passlayer_ref, layerout_ref, step, result_sem.at[1], 4)
    fetch = pltpu.make_async_copy(tokens_ref.at[place.t], own_ref, local_sem.at[0])
    fetch_layer, fetch_work, fetch_fold, fetch_gbt, fetch_a1t = [
        pltpu.make_async_copy(there, here, local_sem.at[1 + j])
        for j, (there, here) in enumerate([
            (layer_in, layer_ref), (work_in, work_ref), (fold_in, fold_ref),
            (gbt_in, gbt_ref), (a1t_in, a1t_ref),
        ])
    ]
    def operands(group):
        slot = group % 2
        pairs = [
            (gw_in, gw_ref), (scale_in, scale_ref), (o_in, o_ref), (v_in, v_ref),
            (q_in, q_ref), (kt_in, kt_ref), (gq_in, gq_ref),
        ]
        return [
            pltpu.make_async_copy(there.at[group], here.at[slot], group_sem.at[slot, j])
            for j, (there, here) in enumerate(pairs)
        ]

    corew = [links.add(place.to_core, stagew_ref, landw_ref.at[i]) for i in range(2)]
    core0 = [links.add(place.to_core, stage0_ref, land0_ref.at[i]) for i in range(2)]
    def half_done(i, *landing):
        return Reduce(
            links, place, lambda s, z, y: work_ref.at[i, z, y],
            lambda s, z: folded_ref.at[i, z] if s else fold_ref.at[i, z],
            *landing, slots=(1,),
        )

    seg1 = half_done(0, cross1_ref, far1_ref, mid1_ref, last1_ref, side1_ref)
    seg2 = half_done(1, cross2_ref, far2_ref, mid2_ref, last2_ref, side2_ref)
    segw = Reduce(
        links, place, lambda s, z, y: workw_ref.at[s, z, y],
        lambda s, z: workw_ref.at[s, z, y],
        crossw_ref, farw_ref, midw_ref, lastw_ref, sidew_ref,
    )
    seg0 = Reduce(
        links, place, lambda s, z, y: work0_ref.at[s, z, y],
        lambda s, z: work0_ref.at[s, z, y],
        cross0_ref, far0_ref, mid0_ref, last0_ref, side0_ref, slots=(0,), split=True,
    )
    tail = ReduceHalves(links, place, work0_ref.at[1], tail_refs, last0_ref)
    sum_core, sum_y, *sum_z, sum_x = [
        links.add(to, sums_ref.at[i], sumland_ref.at[j])
        for j, (i, to) in enumerate(
            zip([0, 1, 2, 2, 2, 3], [place.to_core, place.to_y] + place.to_z[1:] + [place.to_x])
        )
    ]

    early_copies = [
        corew[1], core0[1], *segw.y[0], *segw.y[1], *seg0.y[0], *layer.x, *layer.core,
    ]
    for seg in (seg1, seg2):
        early_copies += [*seg.y[1], *seg.z[0], *seg.z[1]]

    def sent(copies):
        for copy in copies:
            copy.wait_send()

    def when(point):
        return pl.when(t == point)

    @when(0)
    def _():
        start(fetch_layer, operands(1), fetch_work, fetch_fold, fetch_gbt, operands(0))
        start(fetch, fetch_a1t)
        place.greet()
        fetch_layer.wait()
        for i in range(4):
            layer.send(i)
        fetch_work.wait()
        start(seg1.y[1], seg2.y[1])
        fetch_fold.wait()
        start(seg1.z[0][:2], seg2.z[0][:2])
        bqv_ref[...] = jnp.zeros_like(bqv_ref)
        sums_ref[0] = early_ref[...]
        fetch_gbt.wait()

    def add_core():
        recv(corew[1])

        @pl.loop(0, Z_DEV)
        def _(z):
            workw_ref[1, z] = (
                workw_ref[1, z].astype(F32) + landw_ref[1, z].astype(F32)
            ).astype(BF16)

        start(segw.y[1])

    def wait(copies):
        for copy in copies:
            copy.wait()

    @when(0)
    def _():
        wait(operands(1))

    @when(4)
    def _():
        start(operands(3))
        wait(operands(0))

    @when(8)
    def _():
        start(operands(2))
        wait(operands(3))

    @when(9)
    def _():
        wait(operands(2))

    plan = [
        (7, 1, lambda: (seg1.fold_y(1, 0), seg1.fold_z(0), layer.pass_on(0))),
        (8, 1, lambda: (seg1.fold_y(1, 1), seg2.fold_z(0), layer.pass_on(1))),
        (9, 1, add_core),
        (10, 1, lambda: (seg1.fold_z(1), seg2.fold_y(1, 0))),
        (11, 1, lambda: layer.pass_on(2)),
        (12, 1, lambda: (seg2.fold_y(1, 1), seg1.send_x())),
        (14, 1, lambda: (segw.fold_y(0, 0), segw.fold_y(0, 1))),
    ]

    def serve(point):
        for at, where, act in plan:
            if where == point:
                pl.when(t == at)(lambda act=act: (act(), None)[1])

    @pl.when((t == 0) | (t == 4) | (t == 8) | (t == 9))
    def _():
        pick = (
            lax.broadcasted_iota(jnp.int32, (8, width), 1) // HEAD_DIM
            == lax.broadcasted_iota(jnp.int32, (8, width), 0)
        ).astype(BF16)

        @pl.loop(0, n // step)
        def _(i):
            rows = pl.ds(pl.multiple_of(i * step, step), step)
            columns = scale_ref[now, :, rows].T
            lane = lax.broadcasted_iota(jnp.int32, (step, width), 1)
            scale = columns[:, heads - 1 : heads]
            for h in reversed(range(heads - 1)):
                scale = jnp.where(lane < (h + 1) * HEAD_DIM, columns[:, h : h + 1], scale)
            do = (dot_nn(gb_ref[rows, :], gw_ref[now]) * scale).astype(BF16)
            do_ref[now, rows, :] = do
            product = do.astype(F32) * o_ref[now, rows, :].astype(F32)
            high = product.astype(BF16)
            low = (product - high.astype(F32)).astype(BF16)
            delta_ref[now, :, rows] = dot_nt(pick, high) + dot_nt(pick, low)

        value = dot_nn(gbt_ref[...], o_ref[now]).reshape(Z_DEV, Y_DEV, depth, width)
        for s in range(2):
            @when(8 * s)
            def _():
                if s:
                    corew[0].wait_send()
                stagew_ref[...] = value.astype(BF16)
                start(corew[s])

        @when(4)
        def _():
            recv(corew[0])
            workw_ref[0] = (value + landw_ref[0].astype(F32)).astype(BF16)
            start(segw.y[0])

        @when(9)
        def _():
            workw_ref[1] = value.astype(BF16)

    serve(0)

    for ii in reversed(range(4)):
        @pl.when(i == ii)
        def _():
            first, last = ii * step, (ii + 1) * step
            do = do_ref[now, first:last, :]
            q = q_ref[now, first:last, :]
            v = v_ref[now, :last, :]
            lane = lax.broadcasted_iota(jnp.int32, (1, width), 1)
            dk, dv, dq = None, None, []
            for h in range(heads):
                low, high = h * HEAD_DIM, (h + 1) * HEAD_DIM
                here = (lane >= low) & (lane < high)
                p = p_ref[0, h, 0, :last, :]
                dp = dot_nt(v, jnp.where(here, do, jnp.zeros((), BF16)))
                ds = p * (dp - delta_ref[now, h : h + 1, first:last]).astype(BF16)
                part = dot_nn(p, do)
                dv = part if dv is None else jnp.where(lane < low, dv, part)
                part = dot_nn(ds, q)
                dk = part if dk is None else jnp.where(lane < low, dk, part)
                dq.append(dot_nn(kt_ref[now, low:high, :last], ds))
            if ii == 3:
                dkv_ref[now, 0] = dk
                dkv_ref[now, 1] = dv
            else:
                dkv_ref[now, 0, :last, :] += dk
                dkv_ref[now, 1, :last, :] += dv
            dk = dkv_ref[now, 0, first:last, :].astype(BF16)
            dv = dkv_ref[now, 1, first:last, :].astype(BF16)
            dq = (jnp.concatenate(dq, 0) * HEAD_DIM ** -0.5).astype(BF16).T
            dqkv_ref[now, first:last, :width] = dq
            dqkv_ref[now, first:last, width : 2 * width] = dk
            dqkv_ref[now, first:last, 2 * width :] = dv
            bqv_ref[mine, 0:1, :] += jnp.sum(dq.astype(F32), 0, keepdims=True)
            bqv_ref[mine, 1:2, :] += jnp.sum(dv.astype(F32), 0, keepdims=True)

            @pl.when(t >= 8)
            def _():
                da1_ref[first:last, :] += dot_nt(dqkv_ref[now, first:last, :], gq_ref[now])

    serve(1)

    @pl.when((t == 3) | (t == 7) | (t > 13))
    def _():
        @when(3)
        def _():
            fetch.wait()
            fetch_a1t.wait()

        @when(3)
        def _():
            da1_ref[...] = dot_nt(dqkv_ref[now], gq_ref[now])

        @when(7)
        def _():
            da1_ref[...] += dot_nt(dqkv_ref[now], gq_ref[now])

        value = dot_nn(a1t_ref[...], dqkv_ref[now]).reshape(Z_DEV, Y_DEV, depth, 3 * width)
        for s in range(2):
            @when(3 + 11 * s)
            def _():
                if s:
                    core0[0].wait_send()
                stage0_ref[...] = value.astype(BF16)
                start(core0[s])

            @when(7 + 8 * s)
            def _():
                recv(core0[s])
                work0_ref[s] = (value + land0_ref[s].astype(F32)).astype(BF16)
                if s:
                    tail.begin()
                else:
                    start(seg0.y[s])

    @pl.when((t > 8) & (t % 2 == 1))
    def _():
        rows = pl.ds(pl.multiple_of(i * step, step), step)
        xhat, r = norm_parts(own_ref[rows, :].astype(F32))
        da1 = da1_ref[rows, :]
        sums_ref[0, 0:1, :] += jnp.sum(da1 * xhat, 0, keepdims=True)
        sums_ref[0, 2:3, :] += jnp.sum(da1, 0, keepdims=True)
        dg = da1 * rows_ref[0:1, :]
        dv = r * (
            dg
            - jnp.mean(dg, -1, keepdims=True)
            - xhat * jnp.mean(dg * xhat, -1, keepdims=True)
        )
        own_ref[rows, :] = (dh1_ref[...] + dv).astype(BF16)
        for ii in range(4):
            @pl.when(i == ii)
            def _():
                out.send(ii)

    @when(15)
    def _():
        for s in range(4):
            sums_ref[0, 3:5, s * width : (s + 1) * width] = bqv_ref[s, 0:2, :]
        start(sum_core)
        seg2.fold_z(1)
        layer.pass_on(3)
        seg0.fold_y(0, 0)
        seg0.fold_y(0, 1)
        segw.fold_z(0)
        segw.fold_y(1, 0)
        segw.fold_y(1, 1)
        recv(sum_core)
        sums_ref[1] = sums_ref[0] + sumland_ref[0]
        start(sum_y)
        seg2.send_x()
        seg0.fold_z(0)
        out.pass_on(3)
        tail.fold_high()
        segw.fold_z(1)
        sent(early_copies)
        tail.fold_y()
        recv(sum_y)
        sums_ref[2] = sums_ref[1] + sumland_ref[1]
        start(sum_z)
        tail.cross_high()
        segw.send_x()
        tail.fold_z()
        recv(sum_z)
        sums_ref[3] = (sums_ref[2] + sumland_ref[2]) + (sumland_ref[3] + sumland_ref[4])
        start(sum_x)
        tail.finish()
        start(seg0.x)
        out.pass_on(2)
        part1_ref[...] = seg1.total()
        part2_ref[...] = seg2.total()
        out.pass_on(1)
        partw_ref[...] = segw.total()
        layer.finish()
        out.pass_on(0)
        recv(sum_x)
        total_ref[...] = sums_ref[3] + sumland_ref[5]
        part0_ref[...] = seg0.total()
        out.finish()
        links.sent(corew[0], core0[0], *early_copies)


def group_and_block(t):
    early = t < 8
    return (
        jnp.where(early, 1 - t // 4, 3 - t % 2),
        3 - jnp.where(early, t % 4, jnp.maximum(t - 8, 0) // 2),
    )


def run_fused_backward(
    tokens, gq, gw, rows, dh1, gb, gbt, q, v, kt, p, scale, o, a1t, layer, fold, work, early
):
    groups, n, _ = tokens.shape
    width = gw.shape[-1]
    heads = width // HEAD_DIM
    hidden = fold.shape[-1]
    depth = D // (Z_DEV * Y_DEV)
    step = n // 4

    p_spec = pl.BlockSpec(
        (1, heads, 1, n, step),
        lambda t: (group_and_block(t)[0], 0, group_and_block(t)[1], 0, 0),
    )

    copies = 12 + 12 + 4 + 15 + 2 * 11 + 8 + 11 + 6

    def landing(lanes, slots=1):
        return [
            pltpu.VMEM((slots, Z_DEV, depth, lanes), BF16),
            pltpu.VMEM((2, 3, depth, lanes), BF16), pltpu.VMEM((2, 2, depth, lanes), BF16),
            pltpu.VMEM((depth, lanes), BF16), pltpu.VMEM((depth, lanes), BF16),
        ]

    def working(lanes):
        block = (Z_DEV, Y_DEV, depth, lanes)
        return [pltpu.VMEM(block, BF16)] + [pltpu.VMEM((2,) + block, BF16)] * 2

    return pl.pallas_call(
        fused_backward,
        grid=(4 * groups,),
        in_specs=[
            ANY_WHOLE, ANY_WHOLE, ANY_WHOLE, VMEM_WHOLE,
            pl.BlockSpec((step, D), lambda t: (group_and_block(jnp.maximum(t, 8))[1], 0)),
            VMEM_WHOLE, ANY_WHOLE, ANY_WHOLE, ANY_WHOLE, ANY_WHOLE, p_spec,
            ANY_WHOLE, ANY_WHOLE, ANY_WHOLE, ANY_WHOLE, ANY_WHOLE, ANY_WHOLE, VMEM_WHOLE,
        ],
        out_specs=[ANY_WHOLE] * 2 + [VMEM_WHOLE] * 5,
        out_shape=[
            shaped(BF16, groups, n, D), shaped(BF16, groups, n, D),
            shaped(F32, depth, 3 * width),
            shaped(F32, depth, width), shaped(F32, depth, hidden),
            shaped(F32, depth, hidden), shaped(F32, 16, D),
        ],
        scratch_shapes=[
            pltpu.VMEM((2, D, 3 * width), BF16), pltpu.VMEM((2, D, width), BF16),
            pltpu.VMEM((2, n, width), BF16), pltpu.VMEM((2, n, width), BF16),
            pltpu.VMEM((2, width, n), BF16), pltpu.VMEM((2, 8, n), F32),
            pltpu.VMEM((2, n, width), BF16),
            pltpu.VMEM((D, n), BF16), pltpu.VMEM((D, n), BF16), pltpu.VMEM((n, D), BF16),
            pltpu.VMEM((2, Z_DEV, depth, hidden), BF16),
            pltpu.VMEM((2, Z_DEV, Y_DEV, depth, hidden), BF16),
            pltpu.VMEM((2, n, width), BF16),
            pltpu.VMEM((2, 8, n), F32), pltpu.VMEM((2, 2, n, width), F32),
            pltpu.VMEM((2, n, 3 * width), BF16), pltpu.VMEM((n, D), F32),
            pltpu.VMEM((n, D), BF16), pltpu.VMEM((n, D), BF16), pltpu.VMEM((n, D), BF16),
            pltpu.VMEM((groups, 8, width), F32),
        ]
        + [pltpu.VMEM((2, Z_DEV, depth, hidden), BF16)] + landing(hidden) + landing(hidden)
        + working(width) + landing(width, 2)
        + working(3 * width) + landing(3 * width)
        + [
            pltpu.VMEM((4, 16, D), F32), pltpu.VMEM((6, 16, D), F32),
            pltpu.SemaphoreType.DMA((copies,)), pltpu.SemaphoreType.DMA((copies,)),
            pltpu.SemaphoreType.DMA((6,)), pltpu.SemaphoreType.DMA((2, 2, 4)),
            pltpu.SemaphoreType.DMA((2, 7)),
            pltpu.VMEM((Z_DEV, depth // 2, 3 * width), BF16),
            pltpu.VMEM((3, depth // 2, 3 * width), BF16),
            pltpu.VMEM((2, depth // 2, 3 * width), BF16),
            pltpu.VMEM((3, Y_DEV, depth // 2, 3 * width), BF16),
            pltpu.VMEM((2, Y_DEV, depth // 2, 3 * width), BF16),
            pltpu.VMEM((Y_DEV, depth // 2, 3 * width), BF16),
            pltpu.VMEM((depth // 2, 3 * width), BF16),
        ],
        compiler_params=pltpu.CompilerParams(
            vmem_limit_bytes=VMEM_LIMIT, collective_id=2, has_side_effects=True
        ),
        name="fused_backward",
    )(tokens, gq, gw, rows, dh1, gb, gbt, q, v, kt, p, scale, o, a1t, layer, fold, work, early)


def place_gradients(
    tie_ref, sums_ref, part0_ref, partw_ref, part1_ref, part2_ref, near_out_ref,
    near_grad_ref, far_out_ref, far_grad_ref, gains_ref, bias_ref, in_ref, out_ref, expand_ref,
    project_ref,
):
    far_out_ref[...] = near_out_ref[...]
    far_grad_ref[...] = near_grad_ref[...]
    own = gains_ref.shape[-1]
    width = partw_ref.shape[-1]

    @pl.when(pl.program_id(0) == 0)
    def _():
        first = (lax.axis_index("dp") * 4 + lax.axis_index("tensor")) * own
        feature = lax.broadcasted_iota(jnp.int32, (D, 128), 0)
        lane = lax.broadcasted_iota(jnp.int32, (D, 128), 1)
        chosen = ((feature == first + lane) & (lane < own)).astype(F32)
        sums = lax.dot_general(
            sums_ref[...], chosen, (((1,), (0,)), ((), ())),
            precision=lax.Precision.HIGHEST, preferred_element_type=F32,
        )[:, :own]
        s0, s1, s2, s3 = tie_ref[0], tie_ref[1], tie_ref[2], tie_ref[3]
        w_out = partw_ref[...].T

        def at(source, wanted, value):
            return jnp.where(source == wanted, value, jnp.zeros_like(value))

        row = lax.broadcasted_iota(jnp.int32, (NSRC, own), 0)
        for i, wanted in enumerate([s0, s0, s0, s1, s2, s3, s2, s2, s2, s2]):
            bias_ref[i] = jnp.where(row == wanted, sums[2 + i : 3 + i], 0.0)
        for s in range(NSRC):
            gains_ref[s, 0:1] = at(s, s0, sums[0:1])
            gains_ref[s, 1:2] = at(s, s2, sums[1:2])
            for j in range(3):
                in_ref[s, j] = at(s, s0, part0_ref[:, j * width : (j + 1) * width])
            out_ref[s] = at(s, s1, w_out)
            expand_ref[s] = at(s, s2, part1_ref[...])
            project_ref[s] = at(s, s3, part2_ref[...])


def run_place_gradients(tie, sums, part0, partw, part1, part2, out, grad, like):
    slots, n, _ = grad.shape
    gains, biases, w_in, w_out, w_expand, w_project = [item.shape for item in like]
    shapes = [
        gains, (biases[1], biases[0], biases[2]), w_in, w_out, w_expand,
        (w_project[0], w_project[2], w_project[1]),
    ]
    out, grad, gains, biases, w_in, w_out, w_expand, w_project = pl.pallas_call(
        place_gradients,
        grid=(slots,),
        in_specs=[SMEM_WHOLE] + [VMEM_WHOLE] * 5
        + [group(n, D), group(n, D)],
        out_specs=[group(n, D), group(n, D)] + [VMEM_WHOLE] * 6,
        out_shape=[shaped(BF16, slots, n, D)] * 2 + [shaped(F32, *item) for item in shapes],
        compiler_params=pltpu.CompilerParams(vmem_limit_bytes=VMEM_LIMIT),
        name="place_gradients",
    )(tie, sums, part0, partw, part1, part2, out, grad)
    biases = biases.transpose(1, 0, 2)
    return out, grad, gains, biases, w_in, w_out, w_expand, w_project.transpose(0, 2, 1)


def plain_step(
    tokens, lengths, tie_map, norm_gains, bias_rows, attention_in, attention_out,
    expand_weight, project_weight, cotangent,
):
    slot_rows = tokens.shape[0] // lengths.shape[0]
    me = lax.axis_index("tensor")
    in_local = lax.dynamic_index_in_dim(attention_in, tie_map[0], 0, keepdims=False)
    out_local = lax.dynamic_index_in_dim(attention_out, tie_map[1], 0, keepdims=False)
    expand_local = lax.dynamic_index_in_dim(expand_weight, tie_map[2], 0, keepdims=False)
    project_local = lax.dynamic_index_in_dim(project_weight, tie_map[3], 0, keepdims=False)
    local0 = jnp.concatenate([in_local, out_local.T[None]], 0)
    row_kinds = jnp.array([0, 0, 0, 1, 2, 3] + [2] * (FF // D), dtype=jnp.int32)
    gain_kinds = jnp.array([0, 2], dtype=jnp.int32)
    gain_pick = norm_gains[tie_map[gain_kinds], jnp.arange(2)]
    bias_pick = bias_rows[tie_map[row_kinds], jnp.arange(row_kinds.shape[0])]
    vectors = jnp.concatenate([gain_pick, bias_pick], 0)
    x = lax.dynamic_slice_in_dim(tokens, me * slot_rows, slot_rows, 0)
    cot = lax.dynamic_slice_in_dim(cotangent, me * slot_rows, slot_rows, 0)
    length = lax.dynamic_slice_in_dim(lengths, me, 1, 0)
    rows = lax.all_gather(vectors, ("dp", "tensor"), axis=1, tiled=True).astype(F32)
    rows = jnp.concatenate([rows, jnp.zeros((4, D), F32)], 0)

    def gathered(piece, axis):
        piece = lax.all_gather(piece, "dp", axis=axis, tiled=True)
        return lax.all_gather(piece, "tensor", axis=0)

    g0 = gathered(local0, 1)
    g1 = gathered(expand_local, 0)
    g2 = gathered(project_local.T, 0)
    groups, width = g0.shape[0], g0.shape[-1]
    bqv = rows[3:5].reshape(2, groups, width).transpose(1, 0, 2)
    q, v, kt, p, o, a1t, h1, a2, a2t = run_attention_forward(length, x, g0, rows, bqv)
    out, d1, d2, dh1, gb, gbt, sums = run_feed_forward(length, cot, a2, a2t, h1, g1, g2, rows)
    d0, xg, sums_in, sums_qv = run_attention_backward(
        x, g0, rows, dh1, gb, gbt, q, v, kt, p, o, a1t
    )
    layer_out = lax.all_gather(out, "tensor", axis=0, tiled=True)
    tokens_grad = lax.all_gather(xg, "tensor", axis=0, tiled=True)

    def scattered(piece, axis):
        piece = lax.psum_scatter(piece, "tensor", scatter_dimension=0)
        return lax.psum_scatter(piece, "dp", scatter_dimension=axis, tiled=True).astype(F32)

    part0 = scattered(d0, 1)
    part1 = scattered(d1, 0)
    part2 = scattered(d2, 0)
    qv = sums_qv[:, :2].transpose(1, 0, 2).reshape(2, D)
    sums = jnp.concatenate(
        [sums_in[0:1], sums[1:2], sums_in[1:2], qv, sums[5:12]], 0
    )
    sums = lax.psum_scatter(sums, ("dp", "tensor"), scatter_dimension=1, tiled=True)
    return layer_out, tokens_grad, *placed(tie_map, sums, part0, part1, part2)


def fused_step(
    tokens, lengths, tie_map, norm_gains, bias_rows, attention_in, attention_out,
    expand_weight, project_weight, cotangent,
):
    slots = lengths.shape[0]
    tokens = tokens.reshape(slots, -1, D)
    cotangent = cotangent.reshape(slots, -1, D)
    gq, gw, g1, g2, rows, q, v, kt, p, scale, o, a1t, h1, a2, a2t = run_fused_forward(
        tie_map, lengths, tokens, norm_gains, bias_rows, attention_in, attention_out,
        expand_weight, project_weight,
    )
    layer, fold, work, dh1, gb, gbt, early = run_fused_feed_forward(
        lengths, cotangent, a2, a2t, h1, g1, g2, rows
    )
    grad, out, part0, partw, part1, part2, sums = run_fused_backward(
        tokens, gq, gw, rows, dh1, gb, gbt, q, v, kt, p, scale, o, a1t, layer, fold,
        work, early,
    )
    out, grad, *placed_grads = run_place_gradients(
        tie_map, sums, part0, partw, part1, part2, out, grad,
        (norm_gains, bias_rows, attention_in, attention_out, expand_weight, project_weight),
    )
    return out.reshape(-1, D), grad.reshape(-1, D), *placed_grads


def placed(tie_map, sums, part0, part1, part2):
    source = jnp.arange(NSRC, dtype=jnp.int32)

    def place(piece, which):
        pick = (source == tie_map[which]).reshape((NSRC,) + (1,) * piece.ndim)
        return jnp.where(pick, piece[None], 0.0)

    def place_rows(piece, kinds):
        pick = source[:, None] == tie_map[jnp.array(kinds, dtype=jnp.int32)][None, :]
        return jnp.where(pick[:, :, None], piece[None], 0.0)

    return (
        place_rows(sums[:2], [0, 2]),
        place_rows(sums[2:], [0, 0, 0, 1, 2, 3] + [2] * (FF // D)),
        place(part0[:3], 0),
        place(part0[3].T, 1),
        place(part1, 2),
        place(part2.T, 3),
    )


def solution(mesh):
    fused = mesh.shape["dp"] == Z_DEV * Y_DEV and mesh.shape["tensor"] == X_DEV * C_DEV
    return jax.shard_map(
        fused_step if fused else plain_step,
        mesh=mesh,
        in_specs=(
            P("dp", None),
            P("dp"),
            P(),
            P(None, None, ("dp", "tensor")),
            P(None, None, ("dp", "tensor")),
            P(None, None, "dp", "tensor"),
            P(None, "tensor", "dp"),
            P(None, "dp", "tensor"),
            P(None, "tensor", "dp"),
            P("dp", None),
        ),
        out_specs=(
            P("dp", None),
            P("dp", None),
            P(None, None, ("dp", "tensor")),
            P(None, None, ("dp", "tensor")),
            P(None, None, "dp", "tensor"),
            P(None, "tensor", "dp"),
            P(None, "dp", "tensor"),
            P(None, "tensor", "dp"),
        ),
        check_vma=False,
    )
```

```python
import jax
import jax.numpy as jnp
from jax import lax
from jax.experimental import pallas as pl
from jax.experimental.pallas import tpu as pltpu
from jax.sharding import PartitionSpec as P

D = 768
HEAD_DIM = 64
FF = 3072
NSRC = 4
EPS = 1e-05
MASKED = -1e30
F32 = jnp.float32
BF16 = jnp.bfloat16
VMEM_LIMIT = 60 * 1024 * 1024


def dot_nn(a, b):
    return lax.dot_general(a, b, (((1,), (0,)), ((), ())), preferred_element_type=F32)


def dot_nt(a, b):
    return lax.dot_general(a, b, (((1,), (1,)), ((), ())), preferred_element_type=F32)


def norm_parts(v):
    center = jnp.mean(v, -1, keepdims=True)
    centered = v - center
    r = lax.rsqrt(jnp.mean(centered * centered, -1, keepdims=True) + EPS)
    return centered * r, r


def head_mask(shape, h):
    lane = lax.broadcasted_iota(jnp.int32, shape, 1)
    return (lane >= h * HEAD_DIM) & (lane < (h + 1) * HEAD_DIM)


def blocks(total, size):
    return [slice(i * size, (i + 1) * size) for i in range(total // size)]


def attention_forward(
    len_ref, x_ref, g_ref, rows_ref, bqv_ref,
    q_ref, v_ref, kt_ref, p_ref, o_ref, a1t_ref, h1_ref, a2_ref, a2t_ref,
    a1_ref, k_ref, vt_ref, ot_ref, attn_ref,
):
    t = pl.program_id(0)
    n = x_ref.shape[0]
    width = g_ref.shape[-1]
    heads = width // HEAD_DIM
    step = 256
    length = len_ref[0]

    @pl.when(t == 0)
    def _():
        @pl.loop(0, n // step)
        def _(b):
            rows = pl.ds(pl.multiple_of(b * step, step), step)
            xhat, _ = norm_parts(x_ref[rows, :].astype(F32))
            a1 = xhat * rows_ref[0:1, :] + rows_ref[2:3, :]
            a1_ref[rows, :] = a1.astype(BF16)
            a1t_ref[:, rows] = a1.astype(BF16).T
            attn_ref[rows, :] = x_ref[rows, :].astype(F32) + rows_ref[5:6, :]

    @pl.loop(0, n // step)
    def _(b):
        rows = pl.ds(pl.multiple_of(b * step, step), step)
        a1 = a1_ref[rows, :]
        q = (dot_nn(a1, g_ref[0, 0]) + bqv_ref[0, 0:1, :]).astype(BF16)
        q_ref[0, rows, :] = q * jnp.asarray(HEAD_DIM ** -0.5, BF16)
        k = dot_nn(a1, g_ref[0, 1]).astype(BF16)
        k_ref[rows, :] = k
        kt_ref[0, :, rows] = k.T
        v = (dot_nn(a1, g_ref[0, 2]) + bqv_ref[0, 1:2, :]).astype(BF16)
        v_ref[0, rows, :] = v
        vt_ref[:, rows] = v.T

    for h in range(heads):
        k = k_ref[...]
        k = jnp.where(head_mask(k.shape, h), k, jnp.zeros_like(k))
        for b in range(n // step):
            first, last = b * step, (b + 1) * step
            q = q_ref[0, first:last, :]
            key = lax.broadcasted_iota(jnp.int32, (last, step), 0)
            query = lax.broadcasted_iota(jnp.int32, (step, step), 1) + first
            s = dot_nt(k[:last], q)
            near = jnp.where(
                (key[first:] <= query) & (key[first:] < length), s[first:], MASKED
            )
            if b:
                far = jnp.where(key[:first] < length, s[:first], MASKED)
                top = jnp.maximum(
                    jnp.max(far, 0, keepdims=True), jnp.max(near, 0, keepdims=True)
                )
                e_far = jnp.exp(far - top)
                e_near = jnp.exp(near - top)
                total = jnp.sum(e_far, 0, keepdims=True) + jnp.sum(e_near, 0, keepdims=True)
                scale = 1.0 / total
                p_ref[0, h, :first, first:last] = (e_far * scale).astype(BF16)
            else:
                top = jnp.max(near, 0, keepdims=True)
                e_near = jnp.exp(near - top)
                scale = 1.0 / jnp.sum(e_near, 0, keepdims=True)
            p_ref[0, h, first:last, first:last] = (e_near * scale).astype(BF16)
            ot_ref[h * HEAD_DIM : (h + 1) * HEAD_DIM, first:last] = dot_nn(
                vt_ref[h * HEAD_DIM : (h + 1) * HEAD_DIM, :last],
                p_ref[0, h, :last, first:last],
            ).astype(BF16)

    @pl.loop(0, n // step)
    def _(b):
        rows = pl.ds(pl.multiple_of(b * step, step), step)
        o = ot_ref[:, rows].T
        o_ref[0, rows, :] = o
        attn_ref[rows, :] += dot_nt(o, g_ref[0, 3])

    @pl.when(t == pl.num_programs(0) - 1)
    def _():
        @pl.loop(0, n // step)
        def _(b):
            rows = pl.ds(pl.multiple_of(b * step, step), step)
            h1 = attn_ref[rows, :]
            h1_ref[rows, :] = h1
            xhat, _ = norm_parts(h1)
            a2 = (xhat * rows_ref[1:2, :] + rows_ref[6:7, :]).astype(BF16)
            a2_ref[rows, :] = a2
            a2t_ref[:, rows] = a2.T


SQRT_2_PI = 0.7978845608028654


def feed_forward_both(
    len_ref, c_ref, a2_ref, a2t_ref, h1_ref, w1_ref, w2_ref, rows_ref,
    out_ref, d1_ref, d2_ref, dh1_ref, gb_ref, gbt_ref, sums_ref,
    gf_ref, gft_ref, feed_ref, da2_ref, h_ref, df_ref,
):
    t = pl.program_id(0)
    n = c_ref.shape[0]
    step = 256
    length = len_ref[0]

    @pl.when(t == 0)
    def _():
        sums_ref[...] = jnp.zeros_like(sums_ref)

        @pl.loop(0, n // step)
        def _(b):
            rows = pl.ds(pl.multiple_of(b * step, step), step)
            place = b * step + lax.broadcasted_iota(jnp.int32, (step, 1), 0)
            live = (place < length).astype(F32)
            g = (c_ref[rows, :].astype(F32) * live).astype(BF16)
            gf_ref[rows, :] = g
            gft_ref[:, rows] = g.T
            sums_ref[7:8, :] += jnp.sum(g.astype(F32), 0, keepdims=True)

    bias = rows_ref[pl.ds(8 + t, 1), :]

    @pl.loop(0, n // step)
    def _(b):
        rows = pl.ds(pl.multiple_of(b * step, step), step)
        f = dot_nn(a2_ref[rows, :], w1_ref[0]) + bias
        dh = dot_nn(gf_ref[rows, :], w2_ref[0])
        f2 = f * f
        th = jnp.tanh(f * (SQRT_2_PI + (SQRT_2_PI * 0.044715) * f2))
        half = 0.5 + 0.5 * th
        h = (f * half).astype(BF16)
        slope = half + f * (0.5 - 0.5 * th * th) * (
            SQRT_2_PI + (3 * SQRT_2_PI * 0.044715) * f2
        )
        df = (dh * slope).astype(BF16)
        h_ref[rows, :] = h
        df_ref[rows, :] = df
        sums_ref[pl.ds(8 + t, 1), :] += jnp.sum(df.astype(F32), 0, keepdims=True)
        feed = dot_nt(h, w2_ref[0])
        da2 = dot_nt(df, w1_ref[0])

        @pl.when(t == 0)
        def _():
            feed_ref[rows, :] = feed
            da2_ref[rows, :] = da2

        @pl.when(t > 0)
        def _():
            feed_ref[rows, :] += feed
            da2_ref[rows, :] += da2

    @pl.loop(0, D // step)
    def _(b):
        rows = pl.ds(pl.multiple_of(b * step, step), step)
        d1_ref[0, rows, :] = dot_nn(a2t_ref[rows, :], df_ref[...]).astype(BF16)
        d2_ref[0, rows, :] = dot_nn(gft_ref[rows, :], h_ref[...]).astype(BF16)

    @pl.when(t == pl.num_programs(0) - 1)
    def _():
        @pl.loop(0, n // step)
        def _(b):
            rows = pl.ds(pl.multiple_of(b * step, step), step)
            place = b * step + lax.broadcasted_iota(jnp.int32, (step, 1), 0)
            live = (place < length).astype(F32)
            h1 = h1_ref[rows, :]
            out_ref[rows, :] = (live * (h1 + (feed_ref[rows, :] + rows_ref[7:8, :]))).astype(BF16)
            xhat, r = norm_parts(h1)
            da2 = da2_ref[rows, :]
            sums_ref[1:2, :] += jnp.sum(da2 * xhat, 0, keepdims=True)
            sums_ref[6:7, :] += jnp.sum(da2, 0, keepdims=True)
            dg = da2 * rows_ref[1:2, :]
            dv = r * (
                dg
                - jnp.mean(dg, -1, keepdims=True)
                - xhat * jnp.mean(dg * xhat, -1, keepdims=True)
            )
            dh1 = live * c_ref[rows, :].astype(F32) + dv
            dh1_ref[rows, :] = dh1
            gb = dh1.astype(BF16)
            gb_ref[rows, :] = gb
            gbt_ref[:, rows] = gb.T
            sums_ref[5:6, :] += jnp.sum(gb.astype(F32), 0, keepdims=True)


def attention_backward(
    x_ref, g_ref, rows_ref, dh1_ref, gb_ref, gbt_ref, q_ref, v_ref, kt_ref, p_ref,
    o_ref, a1t_ref,
    d0_ref, xg_ref, sums_ref, bqv_ref,
    do_ref, delta_ref, dqt_ref, dq_ref, dk_ref, dv_ref, da1_ref,
):
    t = pl.program_id(0)
    n = x_ref.shape[0]
    width = g_ref.shape[-1]
    heads = width // HEAD_DIM
    step = 256
    pick = (
        lax.broadcasted_iota(jnp.int32, (16, width), 1) // HEAD_DIM
        == lax.broadcasted_iota(jnp.int32, (16, width), 0)
    ).astype(BF16)

    @pl.loop(0, n // step)
    def _(b):
        rows = pl.ds(pl.multiple_of(b * step, step), step)
        do = dot_nn(gb_ref[rows, :], g_ref[0, 3]).astype(BF16)
        do_ref[rows, :] = do
        prod = do.astype(F32) * o_ref[0, rows, :].astype(F32)
        high = prod.astype(BF16)
        low = (prod - high.astype(F32)).astype(BF16)
        delta_ref[:, rows] = dot_nt(pick, high) + dot_nt(pick, low)

    dqt_ref[...] = jnp.zeros_like(dqt_ref)
    for b in range(n // step):
        first, last = b * step, (b + 1) * step
        do = do_ref[first:, :]
        q = q_ref[0, first:, :]
        v = v_ref[0, first:last, :]
        dk, dv = None, None
        for h in range(heads):
            mine = head_mask((1, width), h)
            zero = jnp.zeros((), BF16)
            p = p_ref[0, h, first:last, first:]
            dp = dot_nt(jnp.where(mine, v, zero), do)
            ds = (p.astype(F32) * (dp - delta_ref[h : h + 1, first:])).astype(BF16)
            part = dot_nn(p, jnp.where(mine, do, zero))
            dv = part if dv is None else dv + part
            part = dot_nn(ds, jnp.where(mine, q, zero))
            dk = part if dk is None else dk + part
            head = slice(h * HEAD_DIM, (h + 1) * HEAD_DIM)
            dqt_ref[head, first:] += dot_nn(kt_ref[0, head, first:last], ds)
        dk_ref[first:last, :] = dk.astype(BF16)
        dv_ref[first:last, :] = dv.astype(BF16)

    @pl.when(t == 0)
    def _():
        da1_ref[...] = jnp.zeros_like(da1_ref)

    bqv_ref[...] = jnp.zeros_like(bqv_ref)

    @pl.loop(0, n // step)
    def _(b):
        rows = pl.ds(pl.multiple_of(b * step, step), step)
        dq = (dqt_ref[:, rows] * HEAD_DIM ** -0.5).astype(BF16).T
        dk = dk_ref[rows, :]
        dv = dv_ref[rows, :]
        dq_ref[rows, :] = dq
        bqv_ref[0, 0:1, :] += jnp.sum(dq.astype(F32), 0, keepdims=True)
        bqv_ref[0, 1:2, :] += jnp.sum(dv.astype(F32), 0, keepdims=True)
        da1_ref[rows, :] += (
            dot_nt(dq, g_ref[0, 0]) + dot_nt(dk, g_ref[0, 1]) + dot_nt(dv, g_ref[0, 2])
        )

    @pl.loop(0, D // step)
    def _(b):
        rows = pl.ds(pl.multiple_of(b * step, step), step)
        a1t = a1t_ref[rows, :]
        d0_ref[0, 0, rows, :] = dot_nn(a1t, dq_ref[...]).astype(BF16)
        d0_ref[0, 1, rows, :] = dot_nn(a1t, dk_ref[...]).astype(BF16)
        d0_ref[0, 2, rows, :] = dot_nn(a1t, dv_ref[...]).astype(BF16)
        d0_ref[0, 3, rows, :] = dot_nn(gbt_ref[rows, :], o_ref[0]).astype(BF16)

    @pl.when(t == pl.num_programs(0) - 1)
    def _():
        sums_ref[...] = jnp.zeros_like(sums_ref)

        @pl.loop(0, n // step)
        def _(b):
            rows = pl.ds(pl.multiple_of(b * step, step), step)
            xhat, r = norm_parts(x_ref[rows, :].astype(F32))
            da1 = da1_ref[rows, :]
            sums_ref[0:1, :] += jnp.sum(da1 * xhat, 0, keepdims=True)
            sums_ref[1:2, :] += jnp.sum(da1, 0, keepdims=True)
            dg = da1 * rows_ref[0:1, :]
            dv = r * (
                dg
                - jnp.mean(dg, -1, keepdims=True)
                - xhat * jnp.mean(dg * xhat, -1, keepdims=True)
            )
            xg_ref[rows, :] = (dh1_ref[rows, :] + dv).astype(BF16)


def whole(*shape):
    return pl.BlockSpec(shape, lambda t: (0,) * len(shape))


def group(*shape):
    return pl.BlockSpec((1,) + shape, lambda t: (t,) + (0,) * len(shape))


def shaped(dtype, *shape):
    return jax.ShapeDtypeStruct(shape, dtype)


SMEM_WHOLE = pl.BlockSpec(memory_space=pltpu.SMEM)


def run_attention_forward(length, x, g0, rows, bqv):
    n = x.shape[0]
    groups, _, _, width = g0.shape
    heads = width // HEAD_DIM
    return pl.pallas_call(
        attention_forward,
        grid=(groups,),
        in_specs=[SMEM_WHOLE, whole(n, D), group(4, D, width), whole(16, D), group(2, width)],
        out_specs=[
            group(n, width), group(n, width), group(width, n), group(heads, n, n),
            group(n, width), whole(D, n), whole(n, D), whole(n, D), whole(D, n),
        ],
        out_shape=[
            shaped(BF16, groups, n, width), shaped(BF16, groups, n, width),
            shaped(BF16, groups, width, n), shaped(BF16, groups, heads, n, n),
            shaped(BF16, groups, n, width), shaped(BF16, D, n), shaped(F32, n, D),
            shaped(BF16, n, D), shaped(BF16, D, n),
        ],
        scratch_shapes=[
            pltpu.VMEM((n, D), BF16), pltpu.VMEM((n, width), BF16),
            pltpu.VMEM((width, n), BF16), pltpu.VMEM((width, n), BF16),
            pltpu.VMEM((n, D), F32),
        ],
        compiler_params=pltpu.CompilerParams(vmem_limit_bytes=VMEM_LIMIT),
        name="attention_forward",
    )(length, x, g0, rows, bqv)


def run_feed_forward(length, cot, a2, a2t, h1, g1, g2, rows):
    n = cot.shape[0]
    groups, _, width = g1.shape
    return pl.pallas_call(
        feed_forward_both,
        grid=(groups,),
        in_specs=[
            SMEM_WHOLE, whole(n, D), whole(n, D), whole(D, n), whole(n, D),
            group(D, width), group(D, width), whole(16, D),
        ],
        out_specs=[
            whole(n, D), group(D, width), group(D, width), whole(n, D), whole(n, D),
            whole(D, n), whole(16, D),
        ],
        out_shape=[
            shaped(BF16, n, D), shaped(BF16, groups, D, width), shaped(BF16, groups, D, width),
            shaped(F32, n, D), shaped(BF16, n, D), shaped(BF16, D, n), shaped(F32, 16, D),
        ],
        scratch_shapes=[
            pltpu.VMEM((n, D), BF16), pltpu.VMEM((D, n), BF16), pltpu.VMEM((n, D), F32),
            pltpu.VMEM((n, D), F32), pltpu.VMEM((n, width), BF16), pltpu.VMEM((n, width), BF16),
        ],
        compiler_params=pltpu.CompilerParams(vmem_limit_bytes=VMEM_LIMIT),
        name="feed_forward_both",
    )(length, cot, a2, a2t, h1, g1, g2, rows)


def run_attention_backward(x, g0, rows, dh1, gb, gbt, q, v, kt, p, o, a1t):
    n = x.shape[0]
    groups, _, _, width = g0.shape
    heads = width // HEAD_DIM
    return pl.pallas_call(
        attention_backward,
        grid=(groups,),
        in_specs=[
            whole(n, D), group(4, D, width), whole(16, D), whole(n, D), whole(n, D),
            whole(D, n), group(n, width), group(n, width), group(width, n),
            group(heads, n, n), group(n, width), whole(D, n),
        ],
        out_specs=[group(4, D, width), whole(n, D), whole(8, D), group(8, width)],
        out_shape=[
            shaped(BF16, groups, 4, D, width), shaped(BF16, n, D), shaped(F32, 8, D),
            shaped(F32, groups, 8, width),
        ],
        scratch_shapes=[
            pltpu.VMEM((n, width), BF16), pltpu.VMEM((16, n), F32), pltpu.VMEM((width, n), F32),
            pltpu.VMEM((n, width), BF16), pltpu.VMEM((n, width), BF16),
            pltpu.VMEM((n, width), BF16), pltpu.VMEM((n, D), F32),
        ],
        compiler_params=pltpu.CompilerParams(vmem_limit_bytes=VMEM_LIMIT),
        name="attention_backward",
    )(x, g0, rows, dh1, gb, gbt, q, v, kt, p, o, a1t)


Z_DEV, Y_DEV, X_DEV, C_DEV = 4, 2, 2, 2


class Place:
    def __init__(self):
        dp, self.t = lax.axis_index("dp"), lax.axis_index("tensor")
        self.dp = dp
        self.z, self.y = dp // 2, dp % 2
        self.x, self.c = self.t // 2, self.t % 2
        self.other_y = 1 - self.y
        self.zh, self.zl = self.z // 2, self.z % 2
        self.other_zh, self.other_zl = 1 - self.zh, 1 - self.zl
        self.zs = [
            self.z,
            self.z + 1 - 2 * (self.z % 2),
            self.z + 2 - 4 * (self.z // 2),
            3 - self.z,
        ]
        self.ts = [
            self.t,
            self.t + 1 - 2 * (self.t % 2),
            self.t + 2 - 4 * (self.t // 2),
            3 - self.t,
        ]
        self.to_z = [dict(dp=z * 2 + self.y) for z in self.zs]
        self.to_y = dict(dp=self.z * 2 + self.other_y)
        self.to_x = dict(tensor=self.ts[2])
        self.same_t = self.to_z[1:] + [dict(dp=z * 2 + self.other_y) for z in self.zs]
        self.same_dp = [dict(tensor=t) for t in self.ts[1:]]
        self.to_core = dict(tensor=self.ts[1])

    def group(self, k):
        return lax.select(
            k == 0, self.ts[0],
            lax.select(k == 1, self.ts[1], lax.select(k == 2, self.ts[2], self.ts[3])),
        )

    def greet(self, others=None):
        barrier = pltpu.get_barrier_semaphore()
        others = others or self.to_z[1:] + [self.to_y, self.to_x, self.to_core]
        for device in others:
            pl.semaphore_signal(
                barrier, inc=1, device_id=device, device_id_type=pl.DeviceIdType.MESH
            )
        pl.semaphore_wait(barrier, len(others))


class Links:
    def __init__(self, send_sem, recv_sem):
        self.send_sem, self.recv_sem = send_sem, recv_sem
        self.copies = []

    def add(self, device, src, dst):
        number = len(self.copies)
        copy = pltpu.make_async_remote_copy(
            src_ref=src,
            dst_ref=dst,
            send_sem=self.send_sem.at[number],
            recv_sem=self.recv_sem.at[number],
            device_id=device,
            device_id_type=pl.DeviceIdType.MESH,
        )
        self.copies.append(copy)
        return copy

    def sent(self, *apart):
        for copy in self.copies:
            if all(copy is not other for other in apart):
                copy.wait_send()


def flat(copies):
    for item in copies:
        if isinstance(item, list):
            yield from flat(item)
        else:
            yield item


def start(*copies):
    for copy in flat(copies):
        copy.start()


def recv(*copies):
    for copy in flat(copies):
        copy.wait_recv()


class Gather:
    def __init__(self, links, place, own, full, order, single=True, last=True):
        every = slice(None)
        y, other = place.y, place.other_y

        def same(device, k, yy, to):
            return links.add(device, full(k, every, yy), full(to, every, yy))

        def along_z(k, yy, block):
            here, passed = full(k, place.z, yy), full(k, place.zs[2], yy)
            return [
                links.add(place.to_z[1], block, here),
                links.add(place.to_z[2], block, here),
                links.add(place.to_z[1], passed, passed),
            ]

        self.z = along_z(0, y, own)
        if order == X_Z_Y:
            self.first = [links.add(place.to_x, own, full(2, place.z, y))]
            self.far = along_z(2, y, full(2, place.z, y))
            blocks = [(0, y), (2, y), (0, other), (2, other)]
        else:
            blocks = [(0, y), (0, other), (2, y), (2, other)]
        if order == Y_Z_X:
            self.first = [links.add(place.to_y, own, full(0, place.z, y))]
            self.far = along_z(0, other, full(0, place.z, other))
        if order == Z_Y_X and single:
            self.first = [same(place.to_y, 0, y, 0)]
        if order == Z_Y_X and not single:
            self.first = [links.add(place.to_y, own, full(0, place.z, y))]
            for k in range(1, 4):
                block = full(0, place.zs[k], y)
                self.first.append(links.add(place.to_y, block, block))
        self.second = [
            same(place.to_y, k, yy, k) if order == X_Z_Y else same(place.to_x, k, yy, 2)
            for k, yy in blocks[: 2 if last else 1]
        ]
        if not last:
            blocks = [block for block in blocks if block[0] == 0]
        self.core = [same(place.to_core, k, yy, k + 1) for k, yy in blocks]


Z_Y_X, Y_Z_X, X_Z_Y = range(3)


def fused_forward(
    tie_ref, len_ref, tokens_ref, gains_ref, bias_ref, in_ref, out_ref, expand_ref,
    project_ref,
    gq_ref, gw_ref, flat1_ref, flat2_ref, rows_ref,
    q_ref, v_ref, kt_ref, p_ref, scale_ref, o_ref, a1t_out, h1_out, a2_out, a2t_out,
    own0_ref, ownw_ref, own1_ref, own2_ref, square_ref, vec_ref,
    all0_ref, allw_ref, w1_ref, w2_ref, vecs_ref, bqv_ref, x_ref, a1_ref, k_ref, qa_ref, vt_ref, ot_ref, a1t_ref, h1_ref, a2_ref, a2t_ref,
    send_sem, recv_sem, local_sem, flush_sem, row_sem,
):
    t = pl.program_id(0)
    n, _ = x_ref.shape
    width = allw_ref.shape[-1]
    heads = width // HEAD_DIM
    step = 256
    place = Place()
    length = len_ref[place.t]
    links = Links(send_sem, recv_sem)
    z, y, x, c = place.z, place.y, place.x, place.c
    mine_there = vecs_ref.at[z, y, x, c]
    column = vecs_ref.at[:, :, x, c]
    vec_one = [links.add(device, vec_ref, mine_there) for device in place.same_t]
    vec_two = [links.add(device, column, column) for device in place.same_dp]
    seg0 = Gather(
        links, place, own0_ref, lambda k, z, y: all0_ref.at[k, z, y], Z_Y_X, single=False
    )
    segw = Gather(links, place, ownw_ref, lambda k, z, y: allw_ref.at[k, z, y], Z_Y_X)
    seg1 = Gather(
        links, place, own1_ref, lambda k, z, y: w1_ref.at[k, z, y], Y_Z_X, last=False
    )
    seg2 = Gather(
        links, place, own2_ref, lambda k, z, y: w2_ref.at[k, z, y], X_Z_Y, last=False
    )
    flush = [
        [
            pltpu.make_async_copy(ref.at[k], flat.at[k], flush_sem.at[i, k])
            for k in range(3)
        ]
        for i, (ref, flat) in enumerate([(w1_ref, flat1_ref), (w2_ref, flat2_ref)])
    ]
    put_a1t = pltpu.make_async_copy(a1t_ref, a1t_out, local_sem.at[0])
    put_a2t = pltpu.make_async_copy(a2t_ref, a2t_out, local_sem.at[1])
    puts = []
    for i in range(n // step):
        rows = pl.ds(i * step, step)
        puts.append([
            pltpu.make_async_copy(h1_ref.at[rows], h1_out.at[rows], row_sem.at[0, i]),
            pltpu.make_async_copy(a2_ref.at[rows], a2_out.at[rows], row_sem.at[1, i]),
        ])
    fetch = pltpu.make_async_copy(tokens_ref.at[place.t], x_ref, local_sem.at[2])

    def relay_z(copies):
        recv(copies[1])
        start(copies[2])

    def pass_own(seg):
        recv(seg.z[0], seg.z[2])
        if seg is segw:
            start(seg.first)
        start(seg.second[0], seg.core[0])

    def pass_second(seg):
        recv(seg.second)
        if seg is seg2:
            start(seg.core[1])

    def pass_first(seg):
        recv(seg.first)
        if seg is segw:
            start(seg.second[1], seg.core[1])
        else:
            start(seg.far[1], seg.far[0])

    def pass_far(seg):
        recv(seg.far[0], seg.far[2])
        start(seg.core[1:] if seg is seg1 else [])

    def pass_core(seg, i):
        recv(seg.second[i])
        start(seg.core[2 + i])

    plan = [
        (0, 0, lambda: (pass_own(segw), pass_first(seg1), relay_z(seg2.z), pass_first(seg2))),
        (0, 2, lambda: (pass_first(segw), relay_z(seg1.z), pass_core(seg0, 0))),
        (1, 0, lambda: recv(seg0.core[:2])),
        (1, 1, lambda: relay_z(seg1.far)),
        (1, 2, lambda: (
            pass_core(seg0, 1), recv(segw.core[:2]), pass_core(segw, 0), pass_own(seg2),
        )),
        (2, 1, lambda: relay_z(seg2.far)),
        (2, 2, lambda: (pass_core(segw, 1), pass_own(seg1))),
        (3, 0, lambda: (recv(seg0.core[2:]), pass_far(seg1), flush[0][0].start())),
        (3, 1, lambda: (pass_second(seg2), flush[1][0].start())),
        (3, 2, lambda: (pass_far(seg2), flush[1][2].start(), recv(segw.core[2:]))),
    ]

    def serve(point):
        for step, where, act in plan:
            if where == point:
                pl.when(t == step)(lambda act=act: (act(), None)[1])

    @pl.when(t == 0)
    def _():
        s0, s1, s2, s3 = tie_ref[0], tie_ref[1], tie_ref[2], tie_ref[3]
        fetch.start()
        square_ref[...] = jnp.zeros_like(square_ref)
        gain = gains_ref.shape[-1]
        square_ref[0:1, :gain] = gains_ref[s0].astype(F32)[0:1]
        square_ref[1:2, :gain] = gains_ref[s2].astype(F32)[1:2]
        kinds = [s0, s0, s0, s1, s2, s3, s2, s2, s2, s2]
        for i, source in enumerate(kinds):
            wide = bias_ref[i].astype(F32)
            here = lax.broadcasted_iota(jnp.int32, wide.shape, 0) == source
            square_ref[2 + i : 3 + i, :gain] = jnp.sum(
                jnp.where(here, wide, 0.0), 0, keepdims=True
            )
        vec_ref[...] = square_ref[...].T[:gain]
        for j in range(3):
            own0_ref[:, j * width : (j + 1) * width] = in_ref[s0, j]
        place.greet(place.same_t + place.same_dp)
        start(vec_one, seg0.z[1], seg0.z[0], seg0.first[0])
        vecs_ref[z, y, x, c] = vec_ref[...]
        ones = lax.broadcasted_iota(jnp.int32, (vt_ref.shape[1] - HEAD_DIM, n), 0) == 0
        for h in range(heads):
            vt_ref[h, HEAD_DIM:, :] = ones.astype(BF16)
        all0_ref[0, z, y] = own0_ref[...]
        ownw_ref[...] = out_ref[s1].T
        allw_ref[0, z, y] = ownw_ref[...]
        own1_ref[...] = expand_ref[s2]
        own2_ref[...] = project_ref[s3]
        w1_ref[0, z, y] = own1_ref[...]
        w2_ref[0, z, y] = own2_ref[...]
        recv(vec_one)
        start(vec_two)
        relay_z(seg0.z)
        start(seg0.first[2])
        recv(seg0.z[0])
        start(seg0.first[1], segw.z[1], segw.z[0], seg2.z[1])
        recv(vec_two)
        start(seg2.first)
        vecs = vecs_ref[...].reshape(D, vecs_ref.shape[-1]).T[:16]
        rows_ref[...] = vecs
        recv(seg0.z[2])
        start(seg0.first[3], seg1.first, seg0.second[0], seg0.core[0])
        for k in range(4):
            part = slice(k * width, (k + 1) * width)
            bqv_ref[k, 0:1, :width] = vecs[3:4, part]
            bqv_ref[k, 0:1, width : 2 * width] = jnp.zeros((1, width), F32)
            bqv_ref[k, 0:1, 2 * width :] = vecs[4:5, part]
        fetch.wait()

        @pl.loop(0, n // step)
        def _(b):
            rows = pl.ds(pl.multiple_of(b * step, step), step)
            wide = x_ref[rows, :].astype(F32)
            xhat, _ = norm_parts(wide)
            a1 = (xhat * rows_ref[0:1, :] + rows_ref[2:3, :]).astype(BF16)
            a1_ref[rows, :] = a1
            a1t_ref[:, rows] = a1.T
            h1_ref[rows, :] = wide + rows_ref[5:6, :]

        put_a1t.start()
        relay_z(segw.z)
        start(seg2.z[0], seg1.z[1], seg1.z[0])
        recv(seg0.first)
        start(seg0.second[1], seg0.core[1])

    serve(0)
    gq = all0_ref[t].reshape(D, 3 * width)
    gq_ref[0] = gq
    mine = place.group(t)
    qkv = dot_nn(a1_ref[...], gq) + bqv_ref[mine, 0:1, :]
    q = qkv[:, :width].astype(BF16) * jnp.asarray(HEAD_DIM ** -0.5, BF16)
    k = qkv[:, width : 2 * width].astype(BF16)
    v = qkv[:, 2 * width :].astype(BF16)
    q_ref[0] = q
    kt_ref[0] = k.T
    v_ref[0] = v
    vt = v.T
    for h in range(heads):
        vt_ref[h, :HEAD_DIM, :] = vt[h * HEAD_DIM : (h + 1) * HEAD_DIM]
    spare = k_ref.shape[1] - width
    dead = lax.broadcasted_iota(jnp.int32, (n, spare), 0) >= length
    first_column = lax.broadcasted_iota(jnp.int32, (n, spare), 1) == 0
    k_ref[:, :width] = k
    k_ref[:, width:] = jnp.where(first_column & dead, MASKED, 0.0).astype(BF16)
    qa_ref[:, :width] = q
    qa_ref[:, width:] = jnp.where(first_column, 1.0, 0.0).astype(BF16)

    serve(1)
    def scores(h, b):
        first, last = b * step, (b + 1) * step
        q = qa_ref[first:last, :]
        lane = lax.broadcasted_iota(jnp.int32, (1, q.shape[1]), 1)
        keep = head_mask((1, q.shape[1]), h) | (lane >= width)
        return dot_nt(k_ref[:last, :], jnp.where(keep, q, jnp.zeros((), BF16)))

    def attend(h, b, s):
        first, last = b * step, (b + 1) * step
        key = lax.broadcasted_iota(jnp.int32, (step, step), 0)
        query = lax.broadcasted_iota(jnp.int32, (step, step), 1)
        near = jnp.where(key <= query, s[first:], MASKED)
        top = jnp.max(near, 0, keepdims=True)
        if b:
            far = s[:first]
            top = jnp.maximum(top, jnp.max(far, 0, keepdims=True))
        e_near = jnp.exp((near - top).astype(BF16))
        p_ref[0, h, b, first:last, :] = e_near
        o = dot_nn(vt_ref[h, :, first:last], e_near)
        if b:
            e_far = jnp.exp((far - top).astype(BF16))
            p_ref[0, h, b, :first, :] = e_far
            o += dot_nn(vt_ref[h, :, :first], e_far)
        scale = 1.0 / o[HEAD_DIM : HEAD_DIM + 1]
        scale_ref[0, h : h + 1, first:last] = scale
        ot_ref[h * HEAD_DIM : (h + 1) * HEAD_DIM, first:last] = (
            o[:HEAD_DIM] * scale
        ).astype(BF16)

    scale_ref[0, heads:, :] = jnp.zeros((scale_ref.shape[1] - heads, n), F32)
    ready = [scores(h, 0) for h in range(heads)]
    for b in range(n // step):
        ahead = [scores(h, b + 1) for h in range(heads)] if b + 1 < n // step else None
        for h in range(heads):
            attend(h, b, ready[h])
        ready = ahead
    serve(2)

    gw_ref[0] = allw_ref[t].reshape(gw_ref.shape[1:])
    o = ot_ref[...].T
    o_ref[0] = o
    h1_ref[...] += dot_nt(o, gw_ref[0])

    @pl.when(t == 3)
    def _():
        for i, rows in enumerate(blocks(n, step)):
            xhat, _ = norm_parts(h1_ref[rows, :])
            a2 = (xhat * rows_ref[1:2, :] + rows_ref[6:7, :]).astype(BF16)
            a2_ref[rows, :] = a2
            a2t_ref[:, rows] = a2.T
            for put in puts[i]:
                put.start()
        put_a2t.start()
        recv(seg2.core)
        flush[1][1].start()
        recv(seg1.core)
        flush[0][1].start()
        pass_second(seg1)
        flush[0][2].start()
        links.sent()
        for copies in flush + puts + [[put_a1t, put_a2t]]:
            for copy in copies:
                copy.wait()


N_GATHER = 10 + 13 + 10 + 10 + 10
VMEM_WHOLE = pl.BlockSpec(memory_space=pltpu.VMEM)
ANY_WHOLE = pl.BlockSpec(memory_space=pl.ANY)


def run_fused_forward(tie, lengths, tokens, gains, biases, w_in, w_out, w_expand, w_project):
    groups, n, _ = tokens.shape
    depth, width = w_in.shape[-2:]
    heads = width // HEAD_DIM
    hidden = w_expand.shape[-1]
    w_project = w_project.transpose(0, 2, 1)
    biases = biases.transpose(1, 0, 2)
    own = gains.shape[-1]
    return pl.pallas_call(
        fused_forward,
        grid=(groups,),
        in_specs=[SMEM_WHOLE, SMEM_WHOLE, ANY_WHOLE] + [VMEM_WHOLE] * 6,
        out_specs=[
            group(D, 3 * width), group(D, width), ANY_WHOLE, ANY_WHOLE, VMEM_WHOLE,
            group(n, width), group(n, width), group(width, n), group(heads, n // 256, n, 256),
            group(8, n), group(n, width), ANY_WHOLE, ANY_WHOLE, ANY_WHOLE, ANY_WHOLE,
        ],
        out_shape=[
            shaped(BF16, groups, D, 3 * width), shaped(BF16, groups, D, width),
            shaped(BF16, groups, Z_DEV, Y_DEV, depth, hidden),
            shaped(BF16, groups, Z_DEV, Y_DEV, depth, hidden),
            shaped(F32, 16, D),
            shaped(BF16, groups, n, width), shaped(BF16, groups, n, width),
            shaped(BF16, groups, width, n), shaped(BF16, groups, heads, n // 256, n, 256),
            shaped(F32, groups, 8, n), shaped(BF16, groups, n, width), shaped(BF16, D, n), shaped(F32, n, D),
            shaped(BF16, n, D), shaped(BF16, D, n),
        ],
        scratch_shapes=[
            pltpu.VMEM((depth, 3 * width), BF16), pltpu.VMEM((depth, width), BF16),
            pltpu.VMEM((depth, hidden), BF16), pltpu.VMEM((depth, hidden), BF16),
            pltpu.VMEM((128, 128), F32), pltpu.VMEM((own, 128), F32),
            pltpu.VMEM((groups, Z_DEV, Y_DEV, depth, 3 * width), BF16),
            pltpu.VMEM((groups, Z_DEV, Y_DEV, depth, width), BF16),
            pltpu.VMEM((groups, Z_DEV, Y_DEV, depth, hidden), BF16),
            pltpu.VMEM((groups, Z_DEV, Y_DEV, depth, hidden), BF16),
            pltpu.VMEM((Z_DEV, Y_DEV, X_DEV, C_DEV, own, 128), F32),
            pltpu.VMEM((groups, 8, 3 * width), F32),
            pltpu.VMEM((n, D), BF16), pltpu.VMEM((n, D), BF16), pltpu.VMEM((n, 256), BF16),
            pltpu.VMEM((n, 256), BF16), pltpu.VMEM((heads, HEAD_DIM + 16, n), BF16),
            pltpu.VMEM((width, n), BF16),
            pltpu.VMEM((D, n), BF16), pltpu.VMEM((n, D), F32), pltpu.VMEM((n, D), BF16),
            pltpu.VMEM((D, n), BF16),
            pltpu.SemaphoreType.DMA((N_GATHER,)), pltpu.SemaphoreType.DMA((N_GATHER,)),
            pltpu.SemaphoreType.DMA((3,)), pltpu.SemaphoreType.DMA((2, 4)),
            pltpu.SemaphoreType.DMA((2, n // 256)),
        ],
        compiler_params=pltpu.CompilerParams(
            vmem_limit_bytes=VMEM_LIMIT, collective_id=0, has_side_effects=True
        ),
        name="fused_forward",
    )(tie, lengths, tokens, gains, biases, w_in, w_out, w_expand, w_project)


class Result:
    def __init__(self, links, place, own_ref, passing_ref, out_ref, step, sem, count):
        self.x, self.core, self.far, self.keep, self.keep_far = [], [], [], [], []
        for i in range(count):
            rows = pl.ds(i * step, step)
            mine, theirs = out_ref.at[place.t, rows], out_ref.at[place.ts[2], rows]
            own, passing = own_ref.at[rows], passing_ref.at[rows]
            self.x.append(links.add(place.to_x, own, passing))
            self.core.append(links.add(place.to_core, own, mine))
            self.far.append(links.add(place.to_core, passing, theirs))
            self.keep.append(pltpu.make_async_copy(own, mine, sem.at[0, i]))
            self.keep_far.append(pltpu.make_async_copy(passing, theirs, sem.at[1, i]))

    def send(self, i):
        start(self.x[i], self.core[i], self.keep[i])

    def pass_on(self, i):
        recv(self.x[i])
        start(self.far[i], self.keep_far[i])

    def finish(self):
        recv(self.core, self.far)
        for copy in self.keep + self.keep_far:
            copy.wait()


def low(value):
    return jnp.asarray(value, BF16)


def pair_order(i):
    return i + 1 - 2 * (i % 2)


def fused_feed_forward(
    len_ref, cot_ref, a2_ref, a2t_in, h1_in, far1_ref, far2_ref, rows_ref,
    out_out, fold_ref, work_out, dh1_out, gb_out, gbt_out, sums_ref,
    gf_ref, gft_ref, feed_ref, da2_ref, h_ref, df_ref, weights_ref, missing_ref, third_ref,
    stage_ref, land_ref, near_ref, cross_ref, a2t_ref, h1_ref, out_ref, work_ref, turned_ref,
    send_sem, recv_sem, local_sem, row_sem,
):
    t = pl.program_id(0)
    n = gf_ref.shape[0]
    step = 256
    depth = stage_ref.shape[-2]
    place = Place()
    length = len_ref[place.t]
    links = Links(send_sem, recv_sem)
    y, other = place.y, place.other_y
    last = [
        links.add(place.to_x, far1_ref.at[0, :, other], missing_ref.at[0, 0]),
        links.add(place.to_y, far2_ref.at[2, :, y], missing_ref.at[1, 0]),
    ]
    last_core = [
        links.add(place.to_core, missing_ref.at[i, 0], missing_ref.at[i, 1]) for i in range(2)
    ]
    third = [
        links.add(place.to_core, far_ref.at[2, :, y], third_ref.at[i])
        for i, far_ref in enumerate([far1_ref, far2_ref])
    ]
    core = [
        [links.add(place.to_core, stage_ref.at[i], land_ref.at[s, i]) for i in range(2)]
        for s in range(2)
    ]
    cross = [
        links.add(place.to_y, near_ref.at[i, :, other], cross_ref.at[i]) for i in range(2)
    ]
    fetch = pltpu.make_async_copy(cot_ref.at[place.t], gf_ref, local_sem.at[0])
    gb_ref, gbt_ref, dh1_ref = gf_ref, gft_ref, da2_ref
    late = [
        pltpu.make_async_copy(a2t_in, a2t_ref, local_sem.at[5]),
        pltpu.make_async_copy(h1_in, h1_ref, local_sem.at[6]),
    ]
    puts = []
    for i in range(n // step):
        rows = pl.ds(i * step, step)
        puts.append([
            pltpu.make_async_copy(ref.at[rows], out.at[rows], row_sem.at[j, i])
            for j, (ref, out) in enumerate(
                [(out_ref, out_out), (dh1_ref, dh1_out), (gb_ref, gb_out)]
            )
        ])
    put_gbt = pltpu.make_async_copy(gbt_ref, gbt_out, local_sem.at[7])
    put_work = pltpu.make_async_copy(turned_ref, work_out, local_sem.at[8])
    k = pair_order(t)
    mine = place.group(k)

    def load(step, whole, slot):
        for i, far_ref in enumerate([far1_ref, far2_ref]):
            group = far_ref.at[pair_order(step)]
            to = weights_ref.at[slot, i]
            if not whole:
                group, to = group.at[:, y], to.at[:, y]
            yield pltpu.make_async_copy(group, to, local_sem.at[1 + 2 * slot + i])

    def live_rows(b):
        at = b * step + lax.broadcasted_iota(jnp.int32, (step, 1), 0)
        return (at < length).astype(F32)

    @pl.when(t == 0)
    def _():
        fetch.start()
        for copy in load(0, True, 0):
            copy.start()
        for copy in late:
            copy.start()
        place.greet()
        start(last, third)
        sums_ref[...] = jnp.zeros_like(sums_ref)
        feed_ref[...] = jnp.zeros_like(feed_ref)
        da2_ref[...] = jnp.zeros_like(da2_ref)
        fetch.wait()

        @pl.loop(0, n // step)
        def _(b):
            rows = pl.ds(pl.multiple_of(b * step, step), step)
            g = (gf_ref[rows, :].astype(F32) * live_rows(b)).astype(BF16)
            gf_ref[rows, :] = g
            gft_ref[:, rows] = g.T
            sums_ref[7:8, :] += jnp.sum(g.astype(F32), 0, keepdims=True)

    for i in range(4):
        @pl.when(t == i)
        def _():
            if i == 2:
                recv(last_core, third)
            else:
                for copy in load(i, i < 2, i % 2):
                    copy.wait()
            if i in (0, 2):
                for copy in load(i + 1, i + 1 < 2, (i + 1) % 2):
                    copy.start()
            for j in range(2):
                if i == 2:
                    weights_ref[0, j, :, y] = third_ref[j]
                if i >= 2:
                    weights_ref[i % 2, j, :, other] = missing_ref[j, 3 - i]

    bias = rows_ref[pl.ds(8 + mine, 1), :]
    w1 = weights_ref[t % 2, 0].reshape(D, -1)
    w2 = weights_ref[t % 2, 1].reshape(D, -1)
    column = jnp.zeros((1, w1.shape[1]), F32)
    for rows in blocks(n, step):
        f = (dot_nn(a2_ref[rows, :], w1) + bias).astype(BF16)
        dh = dot_nn(gf_ref[rows, :], w2)
        f2 = f * f
        th = jnp.tanh(f * (low(SQRT_2_PI) + low(SQRT_2_PI * 0.044715) * f2))
        half = low(0.5) + low(0.5) * th
        h = f * half
        slope = half + f * (low(0.5) - low(0.5) * th * th) * (
            low(SQRT_2_PI) + low(3 * SQRT_2_PI * 0.044715) * f2
        )
        df = (dh * slope.astype(F32)).astype(BF16)
        h_ref[rows, :] = h
        df_ref[rows, :] = df
        column += jnp.sum(df.astype(F32), 0, keepdims=True)
        feed_ref[rows, :] += dot_nt(h, w2)
        da2_ref[rows, :] += dot_nt(df, w1)
    sums_ref[pl.ds(8 + mine, 1), :] = column

    @pl.when(t == 1)
    def _():
        recv(last)
        start(last_core)

    @pl.when(t == 0)
    def _():
        late[0].wait()

    def weight_grad(left_ref, right_ref):
        value = dot_nn(left_ref[...], right_ref[...])
        return value.reshape(Z_DEV, Y_DEV, depth, value.shape[-1]).astype(BF16)

    grad1 = weight_grad(a2t_ref, df_ref)
    grad2 = weight_grad(gft_ref, h_ref)

    def put(ref):
        ref[0] = grad1
        ref[1] = grad2

    def reduced(ref):
        return lambda i, s, z: (
            ref[i, z].astype(F32) + land_ref[s, i, z].astype(F32)
        ).astype(BF16)

    @pl.when(t == 0)
    def _():
        put(stage_ref)
        start(core[0])

    @pl.when(t == 1)
    def _():
        put(near_ref)
        recv(core[0])

        @pl.loop(0, Z_DEV)
        def _(z):
            for i in range(2):
                near_ref[i, z] = reduced(near_ref)(i, 0, z)

        start(cross)

    @pl.when(t == 2)
    def _():
        for copy in core[0]:
            copy.wait_send()
        put(stage_ref)
        start(core[1])

    @pl.when(t == 3)
    def _():
        put(work_ref)
        late[1].wait()
        for i, rows in enumerate(blocks(n, step)):
            live = live_rows(i)
            h1 = h1_ref[rows, :]
            out_ref[rows, :] = (live * (h1 + (feed_ref[rows, :] + rows_ref[7:8, :]))).astype(BF16)
            xhat, r = norm_parts(h1)
            da2 = da2_ref[rows, :]
            sums_ref[1:2, :] += jnp.sum(da2 * xhat, 0, keepdims=True)
            sums_ref[6:7, :] += jnp.sum(da2, 0, keepdims=True)
            dg = da2 * rows_ref[1:2, :]
            dv = r * (
                dg
                - jnp.mean(dg, -1, keepdims=True)
                - xhat * jnp.mean(dg * xhat, -1, keepdims=True)
            )
            dh1 = gf_ref[rows, :].astype(F32) + dv
            dh1_ref[rows, :] = dh1
            gb = dh1.astype(BF16)
            gb_ref[rows, :] = gb
            gbt_ref[:, rows] = gb.T
            sums_ref[5:6, :] += jnp.sum(gb.astype(F32), 0, keepdims=True)
            for copy in puts[i]:
                copy.start()
        put_gbt.start()
        recv(core[1])

        @pl.loop(0, Z_DEV)
        def _(z):
            for i in range(2):
                turned_ref[i, z % 2, z // 2] = reduced(work_ref)(i, 1, z)

        put_work.start()
        recv(cross)

        @pl.loop(0, Z_DEV)
        def _(z):
            for i in range(2):
                fold_ref[i, z % 2, z // 2] = (
                    near_ref[i, z, y].astype(F32) + cross_ref[i, z].astype(F32)
                ).astype(BF16)

        links.sent(*core[0])
        for copies in puts + [[put_gbt, put_work]]:
            for copy in copies:
                copy.wait()


def run_fused_feed_forward(lengths, cot, a2, a2t, h1, g1, g2, rows):
    n = cot.shape[1]
    groups, _, _, depth, hidden = g1.shape
    both = (2, Z_DEV, Y_DEV, depth, hidden)
    fold = (2, Z_DEV, depth, hidden)
    return pl.pallas_call(
        fused_feed_forward,
        grid=(groups,),
        in_specs=[SMEM_WHOLE, ANY_WHOLE, VMEM_WHOLE] + [ANY_WHOLE] * 4 + [VMEM_WHOLE],
        out_specs=[ANY_WHOLE, VMEM_WHOLE] + [ANY_WHOLE] * 4 + [VMEM_WHOLE],
        out_shape=[
            shaped(BF16, n, D), shaped(BF16, 2, 2, 2, depth, hidden),
            shaped(BF16, 2, 2, 2, Y_DEV, depth, hidden), shaped(F32, n, D),
            shaped(BF16, n, D), shaped(BF16, D, n), shaped(F32, 16, D),
        ],
        scratch_shapes=[
            pltpu.VMEM((n, D), BF16), pltpu.VMEM((D, n), BF16), pltpu.VMEM((n, D), F32),
            pltpu.VMEM((n, D), F32), pltpu.VMEM((n, hidden), BF16), pltpu.VMEM((n, hidden), BF16),
            pltpu.VMEM((2,) + both, BF16),
            pltpu.VMEM((2,) + fold, BF16), pltpu.VMEM(fold, BF16), pltpu.VMEM(both, BF16),
            pltpu.VMEM((2,) + both, BF16),
            pltpu.VMEM(both, BF16), pltpu.VMEM(fold, BF16),
            pltpu.VMEM((D, n), BF16), pltpu.VMEM((n, D), F32), pltpu.VMEM((n, D), BF16),
            pltpu.VMEM(both, BF16), pltpu.VMEM((2, 2, 2, Y_DEV, depth, hidden), BF16),
            pltpu.SemaphoreType.DMA((12,)), pltpu.SemaphoreType.DMA((12,)),
            pltpu.SemaphoreType.DMA((9,)), pltpu.SemaphoreType.DMA((3, n // 256)),
        ],
        compiler_params=pltpu.CompilerParams(
            vmem_limit_bytes=VMEM_LIMIT, collective_id=1, has_side_effects=True
        ),
        name="fused_feed_forward",
    )(lengths, cot, a2, a2t, h1, g1, g2, rows)
class Reduce:
    def __init__(
        self, links, place, work, acc, cross_ref, far_ref, mid_ref, last_ref, side_ref,
        slots=(0, 1),
    ):
        self.place, self.work, self.acc = place, work, acc
        self.cross_ref, self.far_ref, self.mid_ref = cross_ref, far_ref, mid_ref
        self.last_ref, self.side_ref = last_ref, side_ref
        self.two = len(slots) == 2
        lows = (place.other_zl, place.zl)
        self.y = {
            s: [
                links.add(place.to_y, work(s, low, place.other_y), self.cross(s, low))
                for low in lows
            ]
            for s in slots
        }
        self.z = [
            [
                links.add(place.to_z[1], acc(s, place.other_zl), far_ref.at[s, pl.ds(0, 2)]),
                links.add(place.to_z[2], mid_ref.at[s, place.other_zh], far_ref.at[s, 2]),
            ]
            for s in range(2)
        ]
        self.x = links.add(place.to_x, last_ref, side_ref)

    def cross(self, s, low):
        return self.cross_ref.at[s if self.two else 0, low]

    def fold_y(self, s, half):
        low = (self.place.other_zl, self.place.zl)[half]
        recv(self.y[s][half])
        value = self.work(s, low, self.place.y)[...].astype(F32)
        self.acc(s, low)[...] = (value + self.cross(s, low)[...].astype(F32)).astype(BF16)
        if half == 0:
            start(self.z[s][0])

    def fold_z(self, s):
        recv(self.z[s][0])
        value = self.acc(s, self.place.zl)[...].astype(F32)
        self.mid_ref[s] = (value + self.far_ref[s, 0:2].astype(F32)).astype(BF16)
        start(self.z[s][1])

    def own(self, s):
        recv(self.z[s][1])
        return self.mid_ref[s, self.place.zh].astype(F32) + self.far_ref[s, 2].astype(F32)

    def send_x(self):
        self.last_ref[...] = self.own(1).astype(BF16)
        start(self.x)

    def total(self):
        value = self.own(0)
        recv(self.x)
        return value + self.side_ref[...].astype(F32)


def fused_backward(
    tokens_ref, gq_in, gw_in, rows_ref, dh1_ref, gb_ref, gbt_in, q_in, v_in, kt_in,
    p_ref, scale_in, o_in, a1t_in, layer_in, fold_in, work_in, early_ref,
    out_ref, layerout_ref, part0_ref, partw_ref, part1_ref, part2_ref, total_ref,
    gq_ref, gw_ref, q_ref, v_ref, kt_ref, scale_ref, o_ref,
    a1t_ref, gbt_ref, layer_ref, fold_ref, work_ref, do_ref, delta_ref, dkv_ref, dqkv_ref, da1_ref, own_ref, passing_ref, passlayer_ref, bqv_ref,
    folded_ref, cross1_ref, far1_ref, mid1_ref, last1_ref, side1_ref,
    cross2_ref, far2_ref, mid2_ref, last2_ref, side2_ref,
    stagew_ref, landw_ref, workw_ref, crossw_ref, farw_ref, midw_ref, lastw_ref, sidew_ref,
    stage0_ref, land0_ref, work0_ref, cross0_ref, far0_ref, mid0_ref, last0_ref, side0_ref,
    sums_ref, sumland_ref,
    send_sem, recv_sem, local_sem, result_sem, group_sem,
):
    t = pl.program_id(0)
    n = own_ref.shape[0]
    width = gw_ref.shape[-1]
    depth = part0_ref.shape[0]
    heads = width // HEAD_DIM
    step = n // 4
    place = Place()
    y = place.y
    links = Links(send_sem, recv_sem)
    k, i = group_and_block(t)
    mine = place.group(k)
    now = k % 2
    out = Result(links, place, own_ref, passing_ref, out_ref, step, result_sem.at[0], 4)
    layer = Result(links, place, layer_ref, passlayer_ref, layerout_ref, 2 * step, result_sem.at[1], 2)
    fetch = pltpu.make_async_copy(tokens_ref.at[place.t], own_ref, local_sem.at[0])
    fetch_layer, fetch_work, fetch_fold, fetch_gbt, fetch_a1t = [
        pltpu.make_async_copy(there, here, local_sem.at[1 + j])
        for j, (there, here) in enumerate([
            (layer_in, layer_ref), (work_in, work_ref), (fold_in, fold_ref),
            (gbt_in, gbt_ref), (a1t_in, a1t_ref),
        ])
    ]
    def operands(group):
        slot = group % 2
        pairs = [
            (gw_in, gw_ref), (scale_in, scale_ref), (o_in, o_ref), (v_in, v_ref),
            (q_in, q_ref), (kt_in, kt_ref), (gq_in, gq_ref),
        ]
        return [
            pltpu.make_async_copy(there.at[group], here.at[slot], group_sem.at[slot, j])
            for j, (there, here) in enumerate(pairs)
        ]

    corew = [links.add(place.to_core, stagew_ref, landw_ref.at[i]) for i in range(2)]
    core0 = [links.add(place.to_core, stage0_ref, land0_ref.at[i]) for i in range(2)]
    def half_done(i, *landing):
        return Reduce(
            links, place, lambda s, low, y: work_ref.at[i, low, :, y],
            lambda s, low: folded_ref.at[i, low] if s else fold_ref.at[i, low],
            *landing, slots=(1,),
        )

    def all_here(ref, *landing):
        return Reduce(
            links, place, lambda s, low, y: ref.at[s, low, :, y],
            lambda s, low: ref.at[s, low, :, y], *landing,
        )

    seg1 = half_done(0, cross1_ref, far1_ref, mid1_ref, last1_ref, side1_ref)
    seg2 = half_done(1, cross2_ref, far2_ref, mid2_ref, last2_ref, side2_ref)
    segw = all_here(workw_ref, crossw_ref, farw_ref, midw_ref, lastw_ref, sidew_ref)
    seg0 = all_here(work0_ref, cross0_ref, far0_ref, mid0_ref, last0_ref, side0_ref)
    sum_core, sum_y, *sum_z, sum_x = [
        links.add(to, sums_ref.at[i], sumland_ref.at[j])
        for j, (i, to) in enumerate(
            zip([0, 1, 2, 2, 2, 3], [place.to_core, place.to_y] + place.to_z[1:] + [place.to_x])
        )
    ]

    early_copies = [
        corew[1], core0[1], *segw.y[0], *segw.y[1], *seg0.y[0], out.x[3], out.core[3],
        *layer.x, *layer.core, *layer.far, seg1.x, seg2.x,
    ]
    for seg in (seg1, seg2):
        early_copies += [*seg.y[1], *seg.z[0], *seg.z[1]]

    def sent(copies):
        for copy in copies:
            copy.wait_send()

    def when(point):
        return pl.when(t == point)

    @when(0)
    def _():
        start(fetch_layer, operands(1), fetch_work, fetch_fold, fetch_gbt, operands(0))
        start(fetch, fetch_a1t)
        place.greet()
        fetch_layer.wait()
        for i in range(2):
            layer.send(i)
        fetch_work.wait()
        start(seg1.y[1], seg2.y[1])
        fetch_fold.wait()
        start(seg1.z[0][0], seg2.z[0][0])
        bqv_ref[...] = jnp.zeros_like(bqv_ref)
        sums_ref[0] = early_ref[...]
        fetch_gbt.wait()

    def add_core():
        recv(corew[1])

        for low in range(2):
            workw_ref[1, low] = (
                workw_ref[1, low].astype(F32) + landw_ref[1, low].astype(F32)
            ).astype(BF16)

        start(segw.y[1])

    def wait(copies):
        for copy in copies:
            copy.wait()

    @when(0)
    def _():
        wait(operands(1))

    @when(4)
    def _():
        start(operands(3))
        wait(operands(0))

    @when(8)
    def _():
        start(operands(2))
        wait(operands(3))

    @when(9)
    def _():
        wait(operands(2))

    plan = [
        (2, 1, lambda: (seg1.fold_y(1, 0), seg1.fold_z(0))),
        (4, 0, lambda: (seg1.fold_y(1, 1), seg2.fold_z(0))),
        (5, 1, lambda: (seg1.fold_z(1), seg2.fold_y(1, 0), layer.pass_on(0))),
        (7, 1, lambda: seg1.send_x()),
        (8, 0, lambda: seg2.fold_y(1, 1)),
        (8, 1, lambda: (seg2.fold_z(1), segw.fold_y(0, 0), segw.fold_y(0, 1))),
        (9, 0, add_core),
        (10, 1, lambda: (seg2.send_x(), seg0.fold_y(0, 0), layer.pass_on(1), segw.fold_z(0))),
        (12, 1, lambda: seg0.fold_y(0, 1)),
        (13, 1, lambda: (seg0.fold_z(0), out.pass_on(3), segw.fold_y(1, 0), segw.fold_y(1, 1))),
        (14, 1, lambda: segw.fold_z(1)),
    ]

    def serve(point):
        for at, where, act in plan:
            if where == point:
                pl.when(t == at)(lambda act=act: (act(), None)[1])

    @pl.when((t == 0) | (t == 4) | (t == 8) | (t == 9))
    def _():
        pick = (
            lax.broadcasted_iota(jnp.int32, (8, width), 1) // HEAD_DIM
            == lax.broadcasted_iota(jnp.int32, (8, width), 0)
        ).astype(BF16)

        @pl.loop(0, n // step)
        def _(i):
            rows = pl.ds(pl.multiple_of(i * step, step), step)
            columns = scale_ref[now, :, rows].T
            lane = lax.broadcasted_iota(jnp.int32, (step, width), 1)
            scale = columns[:, heads - 1 : heads]
            for h in reversed(range(heads - 1)):
                scale = jnp.where(lane < (h + 1) * HEAD_DIM, columns[:, h : h + 1], scale)
            do = (dot_nn(gb_ref[rows, :], gw_ref[now]) * scale).astype(BF16)
            do_ref[now, rows, :] = do
            product = do.astype(F32) * o_ref[now, rows, :].astype(F32)
            high = product.astype(BF16)
            low = (product - high.astype(F32)).astype(BF16)
            delta_ref[now, :, rows] = dot_nt(pick, high) + dot_nt(pick, low)

        value = dot_nn(gbt_ref[...], o_ref[now]).reshape(2, 2, Y_DEV, depth, width).swapaxes(0, 1)
        for s in range(2):
            @when(8 * s)
            def _():
                if s:
                    corew[0].wait_send()
                stagew_ref[...] = value.astype(BF16)
                start(corew[s])

        @when(4)
        def _():
            recv(corew[0])
            workw_ref[0] = (value + landw_ref[0].astype(F32)).astype(BF16)
            start(segw.y[0])

        @when(9)
        def _():
            workw_ref[1] = value.astype(BF16)

    serve(0)

    for ii in reversed(range(4)):
        @pl.when(i == ii)
        def _():
            first, last = ii * step, (ii + 1) * step
            do = do_ref[now, first:last, :]
            q = q_ref[now, first:last, :]
            v = v_ref[now, :last, :]
            lane = lax.broadcasted_iota(jnp.int32, (1, width), 1)
            dk, dv, dq = None, None, []
            for h in range(heads):
                low, high = h * HEAD_DIM, (h + 1) * HEAD_DIM
                here = (lane >= low) & (lane < high)
                p = p_ref[0, h, 0, :last, :]
                dp = dot_nt(v, jnp.where(here, do, jnp.zeros((), BF16)))
                ds = p * (dp - delta_ref[now, h : h + 1, first:last]).astype(BF16)
                part = dot_nn(p, do)
                dv = part if dv is None else jnp.where(lane < low, dv, part)
                part = dot_nn(ds, q)
                dk = part if dk is None else jnp.where(lane < low, dk, part)
                dq.append(dot_nn(kt_ref[now, low:high, :last], ds))
            if ii == 3:
                dkv_ref[now, 0] = dk
                dkv_ref[now, 1] = dv
            else:
                dkv_ref[now, 0, :last, :] += dk
                dkv_ref[now, 1, :last, :] += dv
            dk = dkv_ref[now, 0, first:last, :].astype(BF16)
            dv = dkv_ref[now, 1, first:last, :].astype(BF16)
            dq = (jnp.concatenate(dq, 0) * HEAD_DIM ** -0.5).astype(BF16).T
            dqkv_ref[now, first:last, :width] = dq
            dqkv_ref[now, first:last, width : 2 * width] = dk
            dqkv_ref[now, first:last, 2 * width :] = dv
            bqv_ref[mine, 0:1, :] += jnp.sum(dq.astype(F32), 0, keepdims=True)
            bqv_ref[mine, 1:2, :] += jnp.sum(dv.astype(F32), 0, keepdims=True)

            @pl.when(t >= 8)
            def _():
                da1_ref[first:last, :] += dot_nt(dqkv_ref[now, first:last, :], gq_ref[now])

    serve(1)

    @pl.when((t == 3) | (t == 7) | (t > 13))
    def _():
        @when(3)
        def _():
            fetch.wait()
            fetch_a1t.wait()

        @when(3)
        def _():
            da1_ref[...] = dot_nt(dqkv_ref[now], gq_ref[now])

        @when(7)
        def _():
            da1_ref[...] += dot_nt(dqkv_ref[now], gq_ref[now])

        value = dot_nn(a1t_ref[...], dqkv_ref[now]).reshape(
            2, 2, Y_DEV, depth, 3 * width
        ).swapaxes(0, 1)
        for s in range(2):
            @when(3 + 11 * s)
            def _():
                if s:
                    core0[0].wait_send()
                stage0_ref[...] = value.astype(BF16)
                start(core0[s])

            @when(7 + 8 * s)
            def _():
                recv(core0[s])
                work0_ref[s] = (value + land0_ref[s].astype(F32)).astype(BF16)
                start(seg0.y[s])

    @pl.when((t > 8) & (t % 2 == 1))
    def _():
        rows = pl.ds(pl.multiple_of(i * step, step), step)
        xhat, r = norm_parts(own_ref[rows, :].astype(F32))
        da1 = da1_ref[rows, :]
        sums_ref[0, 0:1, :] += jnp.sum(da1 * xhat, 0, keepdims=True)
        sums_ref[0, 2:3, :] += jnp.sum(da1, 0, keepdims=True)
        dg = da1 * rows_ref[0:1, :]
        dv = r * (
            dg
            - jnp.mean(dg, -1, keepdims=True)
            - xhat * jnp.mean(dg * xhat, -1, keepdims=True)
        )
        own_ref[rows, :] = (dh1_ref[...] + dv).astype(BF16)
        for ii in range(4):
            @pl.when(i == ii)
            def _():
                out.send(ii)

    @when(15)
    def _():
        for s in range(4):
            sums_ref[0, 3:5, s * width : (s + 1) * width] = bqv_ref[s, 0:2, :]
        start(sum_core)
        segw.send_x()
        sent(early_copies)
        recv(sum_core)
        sums_ref[1] = sums_ref[0] + sumland_ref[0]
        start(sum_y)
        seg0.fold_y(1, 0)
        recv(sum_y)
        sums_ref[2] = sums_ref[1] + sumland_ref[1]
        start(sum_z)
        seg0.fold_y(1, 1)
        seg0.fold_z(1)
        recv(sum_z)
        sums_ref[3] = (sums_ref[2] + sumland_ref[2]) + (sumland_ref[3] + sumland_ref[4])
        start(sum_x)
        out.pass_on(2)
        seg0.send_x()
        part1_ref[...] = seg1.total()
        part2_ref[...] = seg2.total()
        out.pass_on(1)
        partw_ref[...] = segw.total()
        layer.finish()
        out.pass_on(0)
        recv(sum_x)
        total_ref[...] = sums_ref[3] + sumland_ref[5]
        part0_ref[...] = seg0.total()
        out.finish()
        links.sent(corew[0], core0[0], *early_copies)


def group_and_block(t):
    early = t < 8
    return (
        jnp.where(early, 1 - t // 4, 3 - t % 2),
        3 - jnp.where(early, t % 4, jnp.maximum(t - 8, 0) // 2),
    )


def run_fused_backward(
    tokens, gq, gw, rows, dh1, gb, gbt, q, v, kt, p, scale, o, a1t, layer, fold, work, early
):
    groups, n, _ = tokens.shape
    width = gw.shape[-1]
    heads = width // HEAD_DIM
    hidden = fold.shape[-1]
    depth = D // (Z_DEV * Y_DEV)
    step = n // 4

    p_spec = pl.BlockSpec(
        (1, heads, 1, n, step),
        lambda t: (group_and_block(t)[0], 0, group_and_block(t)[1], 0, 0),
    )

    copies = 12 + 6 + 4 + 2 * 7 + 2 * 9 + 6

    def landing(lanes, slots=1):
        return [
            pltpu.VMEM((slots, 2, 2, depth, lanes), BF16),
            pltpu.VMEM((2, 3, depth, lanes), BF16), pltpu.VMEM((2, 2, depth, lanes), BF16),
            pltpu.VMEM((depth, lanes), BF16), pltpu.VMEM((depth, lanes), BF16),
        ]

    def working(lanes):
        block = (2, 2, Y_DEV, depth, lanes)
        return [pltpu.VMEM(block, BF16)] + [pltpu.VMEM((2,) + block, BF16)] * 2

    return pl.pallas_call(
        fused_backward,
        grid=(4 * groups,),
        in_specs=[
            ANY_WHOLE, ANY_WHOLE, ANY_WHOLE, VMEM_WHOLE,
            pl.BlockSpec((step, D), lambda t: (group_and_block(jnp.maximum(t, 8))[1], 0)),
            VMEM_WHOLE, ANY_WHOLE, ANY_WHOLE, ANY_WHOLE, ANY_WHOLE, p_spec,
            ANY_WHOLE, ANY_WHOLE, ANY_WHOLE, ANY_WHOLE, ANY_WHOLE, ANY_WHOLE, VMEM_WHOLE,
        ],
        out_specs=[ANY_WHOLE] * 2 + [VMEM_WHOLE] * 5,
        out_shape=[
            shaped(BF16, groups, n, D), shaped(BF16, groups, n, D),
            shaped(F32, depth, 3 * width),
            shaped(F32, depth, width), shaped(F32, depth, hidden),
            shaped(F32, depth, hidden), shaped(F32, 16, D),
        ],
        scratch_shapes=[
            pltpu.VMEM((2, D, 3 * width), BF16), pltpu.VMEM((2, D, width), BF16),
            pltpu.VMEM((2, n, width), BF16), pltpu.VMEM((2, n, width), BF16),
            pltpu.VMEM((2, width, n), BF16), pltpu.VMEM((2, 8, n), F32),
            pltpu.VMEM((2, n, width), BF16),
            pltpu.VMEM((D, n), BF16), pltpu.VMEM((D, n), BF16), pltpu.VMEM((n, D), BF16),
            pltpu.VMEM((2, 2, 2, depth, hidden), BF16),
            pltpu.VMEM((2, 2, 2, Y_DEV, depth, hidden), BF16),
            pltpu.VMEM((2, n, width), BF16),
            pltpu.VMEM((2, 8, n), F32), pltpu.VMEM((2, 2, n, width), F32),
            pltpu.VMEM((2, n, 3 * width), BF16), pltpu.VMEM((n, D), F32),
            pltpu.VMEM((n, D), BF16), pltpu.VMEM((n, D), BF16), pltpu.VMEM((n, D), BF16),
            pltpu.VMEM((groups, 8, width), F32),
        ]
        + [pltpu.VMEM((2, 2, 2, depth, hidden), BF16)] + landing(hidden) + landing(hidden)
        + working(width) + landing(width, 2)
        + working(3 * width) + landing(3 * width, 2)
        + [
            pltpu.VMEM((4, 16, D), F32), pltpu.VMEM((6, 16, D), F32),
            pltpu.SemaphoreType.DMA((copies,)), pltpu.SemaphoreType.DMA((copies,)),
            pltpu.SemaphoreType.DMA((6,)), pltpu.SemaphoreType.DMA((2, 2, 4)),
            pltpu.SemaphoreType.DMA((2, 7)),
        ],
        compiler_params=pltpu.CompilerParams(
            vmem_limit_bytes=VMEM_LIMIT, collective_id=2, has_side_effects=True
        ),
        name="fused_backward",
    )(tokens, gq, gw, rows, dh1, gb, gbt, q, v, kt, p, scale, o, a1t, layer, fold, work, early)


def place_gradients(
    tie_ref, sums_ref, part0_ref, partw_ref, part1_ref, part2_ref, near_out_ref,
    near_grad_ref, far_out_ref, far_grad_ref, gains_ref, bias_ref, in_ref, out_ref, expand_ref,
    project_ref,
):
    far_out_ref[...] = near_out_ref[...]
    far_grad_ref[...] = near_grad_ref[...]
    own = gains_ref.shape[-1]
    width = partw_ref.shape[-1]

    @pl.when(pl.program_id(0) == 0)
    def _():
        first = (lax.axis_index("dp") * 4 + lax.axis_index("tensor")) * own
        feature = lax.broadcasted_iota(jnp.int32, (D, 128), 0)
        lane = lax.broadcasted_iota(jnp.int32, (D, 128), 1)
        chosen = ((feature == first + lane) & (lane < own)).astype(F32)
        sums = lax.dot_general(
            sums_ref[...], chosen, (((1,), (0,)), ((), ())),
            precision=lax.Precision.HIGHEST, preferred_element_type=F32,
        )[:, :own]
        s0, s1, s2, s3 = tie_ref[0], tie_ref[1], tie_ref[2], tie_ref[3]
        w_out = partw_ref[...].T

        def at(source, wanted, value):
            return jnp.where(source == wanted, value, jnp.zeros_like(value))

        row = lax.broadcasted_iota(jnp.int32, (NSRC, own), 0)
        for i, wanted in enumerate([s0, s0, s0, s1, s2, s3, s2, s2, s2, s2]):
            bias_ref[i] = jnp.where(row == wanted, sums[2 + i : 3 + i], 0.0)
        for s in range(NSRC):
            gains_ref[s, 0:1] = at(s, s0, sums[0:1])
            gains_ref[s, 1:2] = at(s, s2, sums[1:2])
            for j in range(3):
                in_ref[s, j] = at(s, s0, part0_ref[:, j * width : (j + 1) * width])
            out_ref[s] = at(s, s1, w_out)
            expand_ref[s] = at(s, s2, part1_ref[...])
            project_ref[s] = at(s, s3, part2_ref[...])


def run_place_gradients(tie, sums, part0, partw, part1, part2, out, grad, like):
    slots, n, _ = grad.shape
    gains, biases, w_in, w_out, w_expand, w_project = [item.shape for item in like]
    shapes = [
        gains, (biases[1], biases[0], biases[2]), w_in, w_out, w_expand,
        (w_project[0], w_project[2], w_project[1]),
    ]
    out, grad, gains, biases, w_in, w_out, w_expand, w_project = pl.pallas_call(
        place_gradients,
        grid=(slots,),
        in_specs=[SMEM_WHOLE] + [VMEM_WHOLE] * 5
        + [group(n, D), group(n, D)],
        out_specs=[group(n, D), group(n, D)] + [VMEM_WHOLE] * 6,
        out_shape=[shaped(BF16, slots, n, D)] * 2 + [shaped(F32, *item) for item in shapes],
        compiler_params=pltpu.CompilerParams(vmem_limit_bytes=VMEM_LIMIT),
        name="place_gradients",
    )(tie, sums, part0, partw, part1, part2, out, grad)
    biases = biases.transpose(1, 0, 2)
    return out, grad, gains, biases, w_in, w_out, w_expand, w_project.transpose(0, 2, 1)


def plain_step(
    tokens, lengths, tie_map, norm_gains, bias_rows, attention_in, attention_out,
    expand_weight, project_weight, cotangent,
):
    slot_rows = tokens.shape[0] // lengths.shape[0]
    me = lax.axis_index("tensor")
    in_local = lax.dynamic_index_in_dim(attention_in, tie_map[0], 0, keepdims=False)
    out_local = lax.dynamic_index_in_dim(attention_out, tie_map[1], 0, keepdims=False)
    expand_local = lax.dynamic_index_in_dim(expand_weight, tie_map[2], 0, keepdims=False)
    project_local = lax.dynamic_index_in_dim(project_weight, tie_map[3], 0, keepdims=False)
    local0 = jnp.concatenate([in_local, out_local.T[None]], 0)
    row_kinds = jnp.array([0, 0, 0, 1, 2, 3] + [2] * (FF // D), dtype=jnp.int32)
    gain_kinds = jnp.array([0, 2], dtype=jnp.int32)
    gain_pick = norm_gains[tie_map[gain_kinds], jnp.arange(2)]
    bias_pick = bias_rows[tie_map[row_kinds], jnp.arange(row_kinds.shape[0])]
    vectors = jnp.concatenate([gain_pick, bias_pick], 0)
    x = lax.dynamic_slice_in_dim(tokens, me * slot_rows, slot_rows, 0)
    cot = lax.dynamic_slice_in_dim(cotangent, me * slot_rows, slot_rows, 0)
    length = lax.dynamic_slice_in_dim(lengths, me, 1, 0)
    rows = lax.all_gather(vectors, ("dp", "tensor"), axis=1, tiled=True).astype(F32)
    rows = jnp.concatenate([rows, jnp.zeros((4, D), F32)], 0)

    def gathered(piece, axis):
        piece = lax.all_gather(piece, "dp", axis=axis, tiled=True)
        return lax.all_gather(piece, "tensor", axis=0)

    g0 = gathered(local0, 1)
    g1 = gathered(expand_local, 0)
    g2 = gathered(project_local.T, 0)
    groups, width = g0.shape[0], g0.shape[-1]
    bqv = rows[3:5].reshape(2, groups, width).transpose(1, 0, 2)
    q, v, kt, p, o, a1t, h1, a2, a2t = run_attention_forward(length, x, g0, rows, bqv)
    out, d1, d2, dh1, gb, gbt, sums = run_feed_forward(length, cot, a2, a2t, h1, g1, g2, rows)
    d0, xg, sums_in, sums_qv = run_attention_backward(
        x, g0, rows, dh1, gb, gbt, q, v, kt, p, o, a1t
    )
    layer_out = lax.all_gather(out, "tensor", axis=0, tiled=True)
    tokens_grad = lax.all_gather(xg, "tensor", axis=0, tiled=True)

    def scattered(piece, axis):
        piece = lax.psum_scatter(piece, "tensor", scatter_dimension=0)
        return lax.psum_scatter(piece, "dp", scatter_dimension=axis, tiled=True).astype(F32)

    part0 = scattered(d0, 1)
    part1 = scattered(d1, 0)
    part2 = scattered(d2, 0)
    qv = sums_qv[:, :2].transpose(1, 0, 2).reshape(2, D)
    sums = jnp.concatenate(
        [sums_in[0:1], sums[1:2], sums_in[1:2], qv, sums[5:12]], 0
    )
    sums = lax.psum_scatter(sums, ("dp", "tensor"), scatter_dimension=1, tiled=True)
    return layer_out, tokens_grad, *placed(tie_map, sums, part0, part1, part2)


def fused_step(
    tokens, lengths, tie_map, norm_gains, bias_rows, attention_in, attention_out,
    expand_weight, project_weight, cotangent,
):
    slots = lengths.shape[0]
    tokens = tokens.reshape(slots, -1, D)
    cotangent = cotangent.reshape(slots, -1, D)
    gq, gw, g1, g2, rows, q, v, kt, p, scale, o, a1t, h1, a2, a2t = run_fused_forward(
        tie_map, lengths, tokens, norm_gains, bias_rows, attention_in, attention_out,
        expand_weight, project_weight,
    )
    layer, fold, work, dh1, gb, gbt, early = run_fused_feed_forward(
        lengths, cotangent, a2, a2t, h1, g1, g2, rows
    )
    grad, out, part0, partw, part1, part2, sums = run_fused_backward(
        tokens, gq, gw, rows, dh1, gb, gbt, q, v, kt, p, scale, o, a1t, layer, fold,
        work, early,
    )
    out, grad, *placed_grads = run_place_gradients(
        tie_map, sums, part0, partw, part1, part2, out, grad,
        (norm_gains, bias_rows, attention_in, attention_out, expand_weight, project_weight),
    )
    return out.reshape(-1, D), grad.reshape(-1, D), *placed_grads


def placed(tie_map, sums, part0, part1, part2):
    source = jnp.arange(NSRC, dtype=jnp.int32)

    def place(piece, which):
        pick = (source == tie_map[which]).reshape((NSRC,) + (1,) * piece.ndim)
        return jnp.where(pick, piece[None], 0.0)

    def place_rows(piece, kinds):
        pick = source[:, None] == tie_map[jnp.array(kinds, dtype=jnp.int32)][None, :]
        return jnp.where(pick[:, :, None], piece[None], 0.0)

    return (
        place_rows(sums[:2], [0, 2]),
        place_rows(sums[2:], [0, 0, 0, 1, 2, 3] + [2] * (FF // D)),
        place(part0[:3], 0),
        place(part0[3].T, 1),
        place(part1, 2),
        place(part2.T, 3),
    )


def solution(mesh):
    fused = mesh.shape["dp"] == Z_DEV * Y_DEV and mesh.shape["tensor"] == X_DEV * C_DEV
    return jax.shard_map(
        fused_step if fused else plain_step,
        mesh=mesh,
        in_specs=(
            P("dp", None),
            P("dp"),
            P(),
            P(None, None, ("dp", "tensor")),
            P(None, None, ("dp", "tensor")),
            P(None, None, "dp", "tensor"),
            P(None, "tensor", "dp"),
            P(None, "dp", "tensor"),
            P(None, "tensor", "dp"),
            P("dp", None),
        ),
        out_specs=(
            P("dp", None),
            P("dp", None),
            P(None, None, ("dp", "tensor")),
            P(None, None, ("dp", "tensor")),
            P(None, None, "dp", "tensor"),
            P(None, "tensor", "dp"),
            P(None, "dp", "tensor"),
            P(None, "tensor", "dp"),
        ),
        check_vma=False,
    )
```

```python
import jax
import jax.numpy as jnp
from jax import lax
from jax.experimental import pallas as pl
from jax.experimental.pallas import tpu as pltpu
from jax.sharding import PartitionSpec as P

D = 768
HEAD_DIM = 64
FF = 3072
NSRC = 4
EPS = 1e-05
MASKED = -1e30
F32 = jnp.float32
BF16 = jnp.bfloat16
VMEM_LIMIT = 60 * 1024 * 1024


def dot_nn(a, b):
    return lax.dot_general(a, b, (((1,), (0,)), ((), ())), preferred_element_type=F32)


def dot_nt(a, b):
    return lax.dot_general(a, b, (((1,), (1,)), ((), ())), preferred_element_type=F32)


def norm_parts(v):
    center = jnp.mean(v, -1, keepdims=True)
    centered = v - center
    r = lax.rsqrt(jnp.mean(centered * centered, -1, keepdims=True) + EPS)
    return centered * r, r


def head_mask(shape, h):
    lane = lax.broadcasted_iota(jnp.int32, shape, 1)
    return (lane >= h * HEAD_DIM) & (lane < (h + 1) * HEAD_DIM)


def blocks(total, size):
    return [slice(i * size, (i + 1) * size) for i in range(total // size)]


def attention_forward(
    len_ref, x_ref, g_ref, rows_ref, bqv_ref,
    q_ref, v_ref, kt_ref, p_ref, o_ref, a1t_ref, h1_ref, a2_ref, a2t_ref,
    a1_ref, k_ref, vt_ref, ot_ref, attn_ref,
):
    t = pl.program_id(0)
    n = x_ref.shape[0]
    width = g_ref.shape[-1]
    heads = width // HEAD_DIM
    step = 256
    length = len_ref[0]

    @pl.when(t == 0)
    def _():
        @pl.loop(0, n // step)
        def _(b):
            rows = pl.ds(pl.multiple_of(b * step, step), step)
            xhat, _ = norm_parts(x_ref[rows, :].astype(F32))
            a1 = xhat * rows_ref[0:1, :] + rows_ref[2:3, :]
            a1_ref[rows, :] = a1.astype(BF16)
            a1t_ref[:, rows] = a1.astype(BF16).T
            attn_ref[rows, :] = x_ref[rows, :].astype(F32) + rows_ref[5:6, :]

    @pl.loop(0, n // step)
    def _(b):
        rows = pl.ds(pl.multiple_of(b * step, step), step)
        a1 = a1_ref[rows, :]
        q = (dot_nn(a1, g_ref[0, 0]) + bqv_ref[0, 0:1, :]).astype(BF16)
        q_ref[0, rows, :] = q * jnp.asarray(HEAD_DIM ** -0.5, BF16)
        k = dot_nn(a1, g_ref[0, 1]).astype(BF16)
        k_ref[rows, :] = k
        kt_ref[0, :, rows] = k.T
        v = (dot_nn(a1, g_ref[0, 2]) + bqv_ref[0, 1:2, :]).astype(BF16)
        v_ref[0, rows, :] = v
        vt_ref[:, rows] = v.T

    for h in range(heads):
        k = k_ref[...]
        k = jnp.where(head_mask(k.shape, h), k, jnp.zeros_like(k))
        for b in range(n // step):
            first, last = b * step, (b + 1) * step
            q = q_ref[0, first:last, :]
            key = lax.broadcasted_iota(jnp.int32, (last, step), 0)
            query = lax.broadcasted_iota(jnp.int32, (step, step), 1) + first
            s = dot_nt(k[:last], q)
            near = jnp.where(
                (key[first:] <= query) & (key[first:] < length), s[first:], MASKED
            )
            if b:
                far = jnp.where(key[:first] < length, s[:first], MASKED)
                top = jnp.maximum(
                    jnp.max(far, 0, keepdims=True), jnp.max(near, 0, keepdims=True)
                )
                e_far = jnp.exp(far - top)
                e_near = jnp.exp(near - top)
                total = jnp.sum(e_far, 0, keepdims=True) + jnp.sum(e_near, 0, keepdims=True)
                scale = 1.0 / total
                p_ref[0, h, :first, first:last] = (e_far * scale).astype(BF16)
            else:
                top = jnp.max(near, 0, keepdims=True)
                e_near = jnp.exp(near - top)
                scale = 1.0 / jnp.sum(e_near, 0, keepdims=True)
            p_ref[0, h, first:last, first:last] = (e_near * scale).astype(BF16)
            ot_ref[h * HEAD_DIM : (h + 1) * HEAD_DIM, first:last] = dot_nn(
                vt_ref[h * HEAD_DIM : (h + 1) * HEAD_DIM, :last],
                p_ref[0, h, :last, first:last],
            ).astype(BF16)

    @pl.loop(0, n // step)
    def _(b):
        rows = pl.ds(pl.multiple_of(b * step, step), step)
        o = ot_ref[:, rows].T
        o_ref[0, rows, :] = o
        attn_ref[rows, :] += dot_nt(o, g_ref[0, 3])

    @pl.when(t == pl.num_programs(0) - 1)
    def _():
        @pl.loop(0, n // step)
        def _(b):
            rows = pl.ds(pl.multiple_of(b * step, step), step)
            h1 = attn_ref[rows, :]
            h1_ref[rows, :] = h1
            xhat, _ = norm_parts(h1)
            a2 = (xhat * rows_ref[1:2, :] + rows_ref[6:7, :]).astype(BF16)
            a2_ref[rows, :] = a2
            a2t_ref[:, rows] = a2.T


SQRT_2_PI = 0.7978845608028654


def feed_forward_both(
    len_ref, c_ref, a2_ref, a2t_ref, h1_ref, w1_ref, w2_ref, rows_ref,
    out_ref, d1_ref, d2_ref, dh1_ref, gb_ref, gbt_ref, sums_ref,
    gf_ref, gft_ref, feed_ref, da2_ref, h_ref, df_ref,
):
    t = pl.program_id(0)
    n = c_ref.shape[0]
    step = 256
    length = len_ref[0]

    @pl.when(t == 0)
    def _():
        sums_ref[...] = jnp.zeros_like(sums_ref)

        @pl.loop(0, n // step)
        def _(b):
            rows = pl.ds(pl.multiple_of(b * step, step), step)
            place = b * step + lax.broadcasted_iota(jnp.int32, (step, 1), 0)
            live = (place < length).astype(F32)
            g = (c_ref[rows, :].astype(F32) * live).astype(BF16)
            gf_ref[rows, :] = g
            gft_ref[:, rows] = g.T
            sums_ref[7:8, :] += jnp.sum(g.astype(F32), 0, keepdims=True)

    bias = rows_ref[pl.ds(8 + t, 1), :]

    @pl.loop(0, n // step)
    def _(b):
        rows = pl.ds(pl.multiple_of(b * step, step), step)
        f = dot_nn(a2_ref[rows, :], w1_ref[0]) + bias
        dh = dot_nn(gf_ref[rows, :], w2_ref[0])
        f2 = f * f
        th = jnp.tanh(f * (SQRT_2_PI + (SQRT_2_PI * 0.044715) * f2))
        half = 0.5 + 0.5 * th
        h = (f * half).astype(BF16)
        slope = half + f * (0.5 - 0.5 * th * th) * (
            SQRT_2_PI + (3 * SQRT_2_PI * 0.044715) * f2
        )
        df = (dh * slope).astype(BF16)
        h_ref[rows, :] = h
        df_ref[rows, :] = df
        sums_ref[pl.ds(8 + t, 1), :] += jnp.sum(df.astype(F32), 0, keepdims=True)
        feed = dot_nt(h, w2_ref[0])
        da2 = dot_nt(df, w1_ref[0])

        @pl.when(t == 0)
        def _():
            feed_ref[rows, :] = feed
            da2_ref[rows, :] = da2

        @pl.when(t > 0)
        def _():
            feed_ref[rows, :] += feed
            da2_ref[rows, :] += da2

    @pl.loop(0, D // step)
    def _(b):
        rows = pl.ds(pl.multiple_of(b * step, step), step)
        d1_ref[0, rows, :] = dot_nn(a2t_ref[rows, :], df_ref[...]).astype(BF16)
        d2_ref[0, rows, :] = dot_nn(gft_ref[rows, :], h_ref[...]).astype(BF16)

    @pl.when(t == pl.num_programs(0) - 1)
    def _():
        @pl.loop(0, n // step)
        def _(b):
            rows = pl.ds(pl.multiple_of(b * step, step), step)
            place = b * step + lax.broadcasted_iota(jnp.int32, (step, 1), 0)
            live = (place < length).astype(F32)
            h1 = h1_ref[rows, :]
            out_ref[rows, :] = (live * (h1 + (feed_ref[rows, :] + rows_ref[7:8, :]))).astype(BF16)
            xhat, r = norm_parts(h1)
            da2 = da2_ref[rows, :]
            sums_ref[1:2, :] += jnp.sum(da2 * xhat, 0, keepdims=True)
            sums_ref[6:7, :] += jnp.sum(da2, 0, keepdims=True)
            dg = da2 * rows_ref[1:2, :]
            dv = r * (
                dg
                - jnp.mean(dg, -1, keepdims=True)
                - xhat * jnp.mean(dg * xhat, -1, keepdims=True)
            )
            dh1 = live * c_ref[rows, :].astype(F32) + dv
            dh1_ref[rows, :] = dh1
            gb = dh1.astype(BF16)
            gb_ref[rows, :] = gb
            gbt_ref[:, rows] = gb.T
            sums_ref[5:6, :] += jnp.sum(gb.astype(F32), 0, keepdims=True)


def attention_backward(
    x_ref, g_ref, rows_ref, dh1_ref, gb_ref, gbt_ref, q_ref, v_ref, kt_ref, p_ref,
    o_ref, a1t_ref,
    d0_ref, xg_ref, sums_ref, bqv_ref,
    do_ref, delta_ref, dqt_ref, dq_ref, dk_ref, dv_ref, da1_ref,
):
    t = pl.program_id(0)
    n = x_ref.shape[0]
    width = g_ref.shape[-1]
    heads = width // HEAD_DIM
    step = 256
    pick = (
        lax.broadcasted_iota(jnp.int32, (16, width), 1) // HEAD_DIM
        == lax.broadcasted_iota(jnp.int32, (16, width), 0)
    ).astype(BF16)

    @pl.loop(0, n // step)
    def _(b):
        rows = pl.ds(pl.multiple_of(b * step, step), step)
        do = dot_nn(gb_ref[rows, :], g_ref[0, 3]).astype(BF16)
        do_ref[rows, :] = do
        prod = do.astype(F32) * o_ref[0, rows, :].astype(F32)
        high = prod.astype(BF16)
        low = (prod - high.astype(F32)).astype(BF16)
        delta_ref[:, rows] = dot_nt(pick, high) + dot_nt(pick, low)

    dqt_ref[...] = jnp.zeros_like(dqt_ref)
    for b in range(n // step):
        first, last = b * step, (b + 1) * step
        do = do_ref[first:, :]
        q = q_ref[0, first:, :]
        v = v_ref[0, first:last, :]
        dk, dv = None, None
        for h in range(heads):
            mine = head_mask((1, width), h)
            zero = jnp.zeros((), BF16)
            p = p_ref[0, h, first:last, first:]
            dp = dot_nt(jnp.where(mine, v, zero), do)
            ds = (p.astype(F32) * (dp - delta_ref[h : h + 1, first:])).astype(BF16)
            part = dot_nn(p, jnp.where(mine, do, zero))
            dv = part if dv is None else dv + part
            part = dot_nn(ds, jnp.where(mine, q, zero))
            dk = part if dk is None else dk + part
            head = slice(h * HEAD_DIM, (h + 1) * HEAD_DIM)
            dqt_ref[head, first:] += dot_nn(kt_ref[0, head, first:last], ds)
        dk_ref[first:last, :] = dk.astype(BF16)
        dv_ref[first:last, :] = dv.astype(BF16)

    @pl.when(t == 0)
    def _():
        da1_ref[...] = jnp.zeros_like(da1_ref)

    bqv_ref[...] = jnp.zeros_like(bqv_ref)

    @pl.loop(0, n // step)
    def _(b):
        rows = pl.ds(pl.multiple_of(b * step, step), step)
        dq = (dqt_ref[:, rows] * HEAD_DIM ** -0.5).astype(BF16).T
        dk = dk_ref[rows, :]
        dv = dv_ref[rows, :]
        dq_ref[rows, :] = dq
        bqv_ref[0, 0:1, :] += jnp.sum(dq.astype(F32), 0, keepdims=True)
        bqv_ref[0, 1:2, :] += jnp.sum(dv.astype(F32), 0, keepdims=True)
        da1_ref[rows, :] += (
            dot_nt(dq, g_ref[0, 0]) + dot_nt(dk, g_ref[0, 1]) + dot_nt(dv, g_ref[0, 2])
        )

    @pl.loop(0, D // step)
    def _(b):
        rows = pl.ds(pl.multiple_of(b * step, step), step)
        a1t = a1t_ref[rows, :]
        d0_ref[0, 0, rows, :] = dot_nn(a1t, dq_ref[...]).astype(BF16)
        d0_ref[0, 1, rows, :] = dot_nn(a1t, dk_ref[...]).astype(BF16)
        d0_ref[0, 2, rows, :] = dot_nn(a1t, dv_ref[...]).astype(BF16)
        d0_ref[0, 3, rows, :] = dot_nn(gbt_ref[rows, :], o_ref[0]).astype(BF16)

    @pl.when(t == pl.num_programs(0) - 1)
    def _():
        sums_ref[...] = jnp.zeros_like(sums_ref)

        @pl.loop(0, n // step)
        def _(b):
            rows = pl.ds(pl.multiple_of(b * step, step), step)
            xhat, r = norm_parts(x_ref[rows, :].astype(F32))
            da1 = da1_ref[rows, :]
            sums_ref[0:1, :] += jnp.sum(da1 * xhat, 0, keepdims=True)
            sums_ref[1:2, :] += jnp.sum(da1, 0, keepdims=True)
            dg = da1 * rows_ref[0:1, :]
            dv = r * (
                dg
                - jnp.mean(dg, -1, keepdims=True)
                - xhat * jnp.mean(dg * xhat, -1, keepdims=True)
            )
            xg_ref[rows, :] = (dh1_ref[rows, :] + dv).astype(BF16)


def whole(*shape):
    return pl.BlockSpec(shape, lambda t: (0,) * len(shape))


def group(*shape):
    return pl.BlockSpec((1,) + shape, lambda t: (t,) + (0,) * len(shape))


def shaped(dtype, *shape):
    return jax.ShapeDtypeStruct(shape, dtype)


SMEM_WHOLE = pl.BlockSpec(memory_space=pltpu.SMEM)


def run_attention_forward(length, x, g0, rows, bqv):
    n = x.shape[0]
    groups, _, _, width = g0.shape
    heads = width // HEAD_DIM
    return pl.pallas_call(
        attention_forward,
        grid=(groups,),
        in_specs=[SMEM_WHOLE, whole(n, D), group(4, D, width), whole(16, D), group(2, width)],
        out_specs=[
            group(n, width), group(n, width), group(width, n), group(heads, n, n),
            group(n, width), whole(D, n), whole(n, D), whole(n, D), whole(D, n),
        ],
        out_shape=[
            shaped(BF16, groups, n, width), shaped(BF16, groups, n, width),
            shaped(BF16, groups, width, n), shaped(BF16, groups, heads, n, n),
            shaped(BF16, groups, n, width), shaped(BF16, D, n), shaped(F32, n, D),
            shaped(BF16, n, D), shaped(BF16, D, n),
        ],
        scratch_shapes=[
            pltpu.VMEM((n, D), BF16), pltpu.VMEM((n, width), BF16),
            pltpu.VMEM((width, n), BF16), pltpu.VMEM((width, n), BF16),
            pltpu.VMEM((n, D), F32),
        ],
        compiler_params=pltpu.CompilerParams(vmem_limit_bytes=VMEM_LIMIT),
        name="attention_forward",
    )(length, x, g0, rows, bqv)


def run_feed_forward(length, cot, a2, a2t, h1, g1, g2, rows):
    n = cot.shape[0]
    groups, _, width = g1.shape
    return pl.pallas_call(
        feed_forward_both,
        grid=(groups,),
        in_specs=[
            SMEM_WHOLE, whole(n, D), whole(n, D), whole(D, n), whole(n, D),
            group(D, width), group(D, width), whole(16, D),
        ],
        out_specs=[
            whole(n, D), group(D, width), group(D, width), whole(n, D), whole(n, D),
            whole(D, n), whole(16, D),
        ],
        out_shape=[
            shaped(BF16, n, D), shaped(BF16, groups, D, width), shaped(BF16, groups, D, width),
            shaped(F32, n, D), shaped(BF16, n, D), shaped(BF16, D, n), shaped(F32, 16, D),
        ],
        scratch_shapes=[
            pltpu.VMEM((n, D), BF16), pltpu.VMEM((D, n), BF16), pltpu.VMEM((n, D), F32),
            pltpu.VMEM((n, D), F32), pltpu.VMEM((n, width), BF16), pltpu.VMEM((n, width), BF16),
        ],
        compiler_params=pltpu.CompilerParams(vmem_limit_bytes=VMEM_LIMIT),
        name="feed_forward_both",
    )(length, cot, a2, a2t, h1, g1, g2, rows)


def run_attention_backward(x, g0, rows, dh1, gb, gbt, q, v, kt, p, o, a1t):
    n = x.shape[0]
    groups, _, _, width = g0.shape
    heads = width // HEAD_DIM
    return pl.pallas_call(
        attention_backward,
        grid=(groups,),
        in_specs=[
            whole(n, D), group(4, D, width), whole(16, D), whole(n, D), whole(n, D),
            whole(D, n), group(n, width), group(n, width), group(width, n),
            group(heads, n, n), group(n, width), whole(D, n),
        ],
        out_specs=[group(4, D, width), whole(n, D), whole(8, D), group(8, width)],
        out_shape=[
            shaped(BF16, groups, 4, D, width), shaped(BF16, n, D), shaped(F32, 8, D),
            shaped(F32, groups, 8, width),
        ],
        scratch_shapes=[
            pltpu.VMEM((n, width), BF16), pltpu.VMEM((16, n), F32), pltpu.VMEM((width, n), F32),
            pltpu.VMEM((n, width), BF16), pltpu.VMEM((n, width), BF16),
            pltpu.VMEM((n, width), BF16), pltpu.VMEM((n, D), F32),
        ],
        compiler_params=pltpu.CompilerParams(vmem_limit_bytes=VMEM_LIMIT),
        name="attention_backward",
    )(x, g0, rows, dh1, gb, gbt, q, v, kt, p, o, a1t)


Z_DEV, Y_DEV, X_DEV, C_DEV = 4, 2, 2, 2


class Place:
    def __init__(self):
        dp, self.t = lax.axis_index("dp"), lax.axis_index("tensor")
        self.dp = dp
        self.z, self.y = dp // 2, dp % 2
        self.x, self.c = self.t // 2, self.t % 2
        self.other_y = 1 - self.y
        self.zs = [
            self.z,
            self.z + 1 - 2 * (self.z % 2),
            self.z + 2 - 4 * (self.z // 2),
            3 - self.z,
        ]
        self.ts = [
            self.t,
            self.t + 1 - 2 * (self.t % 2),
            self.t + 2 - 4 * (self.t // 2),
            3 - self.t,
        ]
        self.to_z = [dict(dp=z * 2 + self.y) for z in self.zs]
        self.to_y = dict(dp=self.z * 2 + self.other_y)
        self.to_x = dict(tensor=self.ts[2])
        self.same_t = self.to_z[1:] + [dict(dp=z * 2 + self.other_y) for z in self.zs]
        self.same_dp = [dict(tensor=t) for t in self.ts[1:]]
        self.to_core = dict(tensor=self.ts[1])

    def group(self, k):
        return lax.select(
            k == 0, self.ts[0],
            lax.select(k == 1, self.ts[1], lax.select(k == 2, self.ts[2], self.ts[3])),
        )

    def greet(self, others=None):
        barrier = pltpu.get_barrier_semaphore()
        others = others or self.to_z[1:] + [self.to_y, self.to_x, self.to_core]
        for device in others:
            pl.semaphore_signal(
                barrier, inc=1, device_id=device, device_id_type=pl.DeviceIdType.MESH
            )
        pl.semaphore_wait(barrier, len(others))


class Pieces:
    def __init__(self, whole, pieces):
        self.whole, self.pieces = whole, pieces

    def start(self):
        for piece in self.pieces:
            piece.start()

    def wait_recv(self):
        self.whole.wait_recv()

    def wait_send(self):
        self.whole.wait_send()


class Links:
    def __init__(self, send_sem, recv_sem):
        self.send_sem, self.recv_sem = send_sem, recv_sem
        self.copies = []

    def add(self, device, src, dst, parts=1, axis=0):
        number = len(self.copies)

        def make(src, dst):
            return pltpu.make_async_remote_copy(
                src_ref=src,
                dst_ref=dst,
                send_sem=self.send_sem.at[number],
                recv_sem=self.recv_sem.at[number],
                device_id=device,
                device_id_type=pl.DeviceIdType.MESH,
            )

        size = src.shape[axis] // parts
        cuts = [(slice(None),) * axis + (pl.ds(i * size, size),) for i in range(parts)]
        copy = Pieces(make(src, dst), [make(src.at[cut], dst.at[cut]) for cut in cuts])
        self.copies.append(copy)
        return copy

    def sent(self, *apart):
        for copy in self.copies:
            if all(copy is not other for other in apart):
                copy.wait_send()


def flat(copies):
    for item in copies:
        if isinstance(item, list):
            yield from flat(item)
        else:
            yield item


def start(*copies):
    for copy in flat(copies):
        copy.start()


def recv(*copies):
    for copy in flat(copies):
        copy.wait_recv()


class Gather:
    def __init__(self, links, place, own, full, order, single=True, last=True):
        every = slice(None)
        y, other = place.y, place.other_y

        def same(device, k, yy, to):
            return links.add(device, full(k, every, yy), full(to, every, yy), Z_DEV)

        def along_z(k, yy, block):
            here, passed = full(k, place.z, yy), full(k, place.zs[2], yy)
            return [
                links.add(place.to_z[1], block, here, 2),
                links.add(place.to_z[2], block, here, 2),
                links.add(place.to_z[1], passed, passed, 2),
            ]

        self.z = along_z(0, y, own)
        if order == X_Z_Y:
            self.first = [links.add(place.to_x, own, full(2, place.z, y), 2)]
            self.far = along_z(2, y, full(2, place.z, y))
            blocks = [(0, y), (2, y), (0, other), (2, other)]
        else:
            blocks = [(0, y), (0, other), (2, y), (2, other)]
        if order == Y_Z_X:
            self.first = [links.add(place.to_y, own, full(0, place.z, y), 2)]
            self.far = along_z(0, other, full(0, place.z, other))
        if order == Z_Y_X and single:
            self.first = [same(place.to_y, 0, y, 0)]
        if order == Z_Y_X and not single:
            self.first = [links.add(place.to_y, own, full(0, place.z, y), 2)]
            for k in range(1, 4):
                block = full(0, place.zs[k], y)
                self.first.append(links.add(place.to_y, block, block, 2))
        self.second = [
            same(place.to_y, k, yy, k) if order == X_Z_Y else same(place.to_x, k, yy, 2)
            for k, yy in blocks[: 2 if last else 1]
        ]
        if not last:
            blocks = [block for block in blocks if block[0] == 0]
        self.core = [same(place.to_core, k, yy, k + 1) for k, yy in blocks]


Z_Y_X, Y_Z_X, X_Z_Y = range(3)


def fused_forward(
    tie_ref, len_ref, tokens_ref, gains_ref, bias_ref, in_ref, out_ref, expand_ref,
    project_ref,
    gq_ref, gw_ref, flat1_ref, flat2_ref, rows_ref,
    q_ref, v_ref, kt_ref, p_ref, scale_ref, o_ref, a1t_out, h1_out, a2_out, a2t_out,
    own0_ref, ownw_ref, own1_ref, own2_ref, square_ref, vec_ref,
    all0_ref, allw_ref, w1_ref, w2_ref, vecs_ref, bqv_ref, x_ref, a1_ref, k_ref, qa_ref, vt_ref, ot_ref, a1t_ref, h1_ref, a2_ref, a2t_ref,
    send_sem, recv_sem, local_sem, flush_sem, row_sem,
):
    t = pl.program_id(0)
    n, _ = x_ref.shape
    width = allw_ref.shape[-1]
    heads = width // HEAD_DIM
    step = 256
    place = Place()
    length = len_ref[place.t]
    links = Links(send_sem, recv_sem)
    z, y, x, c = place.z, place.y, place.x, place.c
    mine_there = vecs_ref.at[z, y, x, c]
    column = vecs_ref.at[:, :, x, c]
    vec_one = [links.add(device, vec_ref, mine_there) for device in place.same_t]
    vec_two = [links.add(device, column, column) for device in place.same_dp]
    seg0 = Gather(
        links, place, own0_ref, lambda k, z, y: all0_ref.at[k, z, y], Z_Y_X, single=False
    )
    segw = Gather(links, place, ownw_ref, lambda k, z, y: allw_ref.at[k, z, y], Z_Y_X)
    seg1 = Gather(
        links, place, own1_ref, lambda k, z, y: w1_ref.at[k, z, y], Y_Z_X, last=False
    )
    seg2 = Gather(
        links, place, own2_ref, lambda k, z, y: w2_ref.at[k, z, y], X_Z_Y, last=False
    )
    flush = [
        [
            pltpu.make_async_copy(ref.at[k], flat.at[k], flush_sem.at[i, k])
            for k in range(3)
        ]
        for i, (ref, flat) in enumerate([(w1_ref, flat1_ref), (w2_ref, flat2_ref)])
    ]
    put_a1t = pltpu.make_async_copy(a1t_ref, a1t_out, local_sem.at[0])
    put_a2t = pltpu.make_async_copy(a2t_ref, a2t_out, local_sem.at[1])
    puts = []
    for i in range(n // step):
        rows = pl.ds(i * step, step)
        puts.append([
            pltpu.make_async_copy(h1_ref.at[rows], h1_out.at[rows], row_sem.at[0, i]),
            pltpu.make_async_copy(a2_ref.at[rows], a2_out.at[rows], row_sem.at[1, i]),
        ])
    fetch = pltpu.make_async_copy(tokens_ref.at[place.t], x_ref, local_sem.at[2])

    def relay_z(copies):
        recv(copies[1])
        start(copies[2])

    def pass_own(seg):
        recv(seg.z[0], seg.z[2])
        if seg is segw:
            start(seg.first)
        start(seg.second[0], seg.core[0])

    def pass_second(seg):
        recv(seg.second)
        if seg is seg2:
            start(seg.core[1])

    def pass_first(seg):
        recv(seg.first)
        if seg is segw:
            start(seg.second[1], seg.core[1])
        else:
            start(seg.far[1], seg.far[0])

    def pass_far(seg):
        recv(seg.far[0], seg.far[2])
        start(seg.core[1:] if seg is seg1 else [])

    def pass_core(seg, i):
        recv(seg.second[i])
        start(seg.core[2 + i])

    plan = [
        (0, 0, lambda: (pass_own(segw), pass_first(seg1), relay_z(seg2.z), pass_first(seg2))),
        (0, 2, lambda: (pass_first(segw), relay_z(seg1.z), pass_core(seg0, 0))),
        (1, 0, lambda: recv(seg0.core[:2])),
        (1, 1, lambda: relay_z(seg1.far)),
        (1, 2, lambda: (
            pass_core(seg0, 1), recv(segw.core[:2]), pass_core(segw, 0), pass_own(seg2),
        )),
        (2, 1, lambda: relay_z(seg2.far)),
        (2, 2, lambda: (pass_core(segw, 1), pass_own(seg1))),
        (3, 0, lambda: (recv(seg0.core[2:]), pass_far(seg1), flush[0][0].start())),
        (3, 1, lambda: (pass_second(seg2), flush[1][0].start())),
        (3, 2, lambda: (pass_far(seg2), flush[1][2].start(), recv(segw.core[2:]))),
    ]

    def serve(point):
        for step, where, act in plan:
            if where == point:
                pl.when(t == step)(lambda act=act: (act(), None)[1])

    @pl.when(t == 0)
    def _():
        s0, s1, s2, s3 = tie_ref[0], tie_ref[1], tie_ref[2], tie_ref[3]
        fetch.start()
        square_ref[...] = jnp.zeros_like(square_ref)
        gain = gains_ref.shape[-1]
        square_ref[0:1, :gain] = gains_ref[s0].astype(F32)[0:1]
        square_ref[1:2, :gain] = gains_ref[s2].astype(F32)[1:2]
        kinds = [s0, s0, s0, s1, s2, s3, s2, s2, s2, s2]
        for i, source in enumerate(kinds):
            wide = bias_ref[i].astype(F32)
            here = lax.broadcasted_iota(jnp.int32, wide.shape, 0) == source
            square_ref[2 + i : 3 + i, :gain] = jnp.sum(
                jnp.where(here, wide, 0.0), 0, keepdims=True
            )
        vec_ref[...] = square_ref[...].T[:gain]
        for j in range(3):
            own0_ref[:, j * width : (j + 1) * width] = in_ref[s0, j]
        place.greet(place.same_t + place.same_dp)
        start(vec_one, seg0.z[1], seg0.z[0], seg0.first[0])
        vecs_ref[z, y, x, c] = vec_ref[...]
        ones = lax.broadcasted_iota(jnp.int32, (vt_ref.shape[1] - HEAD_DIM, n), 0) == 0
        for h in range(heads):
            vt_ref[h, HEAD_DIM:, :] = ones.astype(BF16)
        all0_ref[0, z, y] = own0_ref[...]
        ownw_ref[...] = out_ref[s1].T
        allw_ref[0, z, y] = ownw_ref[...]
        own1_ref[...] = expand_ref[s2]
        own2_ref[...] = project_ref[s3]
        w1_ref[0, z, y] = own1_ref[...]
        w2_ref[0, z, y] = own2_ref[...]
        recv(vec_one)
        start(vec_two)
        relay_z(seg0.z)
        start(seg0.first[2])
        recv(seg0.z[0])
        start(seg0.first[1], segw.z[1], segw.z[0], seg2.z[1])
        recv(vec_two)
        start(seg2.first)
        vecs = vecs_ref[...].reshape(D, vecs_ref.shape[-1]).T[:16]
        rows_ref[...] = vecs
        recv(seg0.z[2])
        start(seg0.first[3], seg1.first, seg0.second[0], seg0.core[0])
        for k in range(4):
            part = slice(k * width, (k + 1) * width)
            bqv_ref[k, 0:1, :width] = vecs[3:4, part]
            bqv_ref[k, 0:1, width : 2 * width] = jnp.zeros((1, width), F32)
            bqv_ref[k, 0:1, 2 * width :] = vecs[4:5, part]
        fetch.wait()

        @pl.loop(0, n // step)
        def _(b):
            rows = pl.ds(pl.multiple_of(b * step, step), step)
            wide = x_ref[rows, :].astype(F32)
            xhat, _ = norm_parts(wide)
            a1 = (xhat * rows_ref[0:1, :] + rows_ref[2:3, :]).astype(BF16)
            a1_ref[rows, :] = a1
            a1t_ref[:, rows] = a1.T
            h1_ref[rows, :] = wide + rows_ref[5:6, :]

        put_a1t.start()
        relay_z(segw.z)
        start(seg2.z[0], seg1.z[1], seg1.z[0])
        recv(seg0.first)
        start(seg0.second[1], seg0.core[1])

    serve(0)
    gq = all0_ref[t].reshape(D, 3 * width)
    gq_ref[0] = gq
    mine = place.group(t)
    qkv = dot_nn(a1_ref[...], gq) + bqv_ref[mine, 0:1, :]
    q = qkv[:, :width].astype(BF16) * jnp.asarray(HEAD_DIM ** -0.5, BF16)
    k = qkv[:, width : 2 * width].astype(BF16)
    v = qkv[:, 2 * width :].astype(BF16)
    q_ref[0] = q
    kt_ref[0] = k.T
    v_ref[0] = v
    vt = v.T
    for h in range(heads):
        vt_ref[h, :HEAD_DIM, :] = vt[h * HEAD_DIM : (h + 1) * HEAD_DIM]
    spare = k_ref.shape[1] - width
    dead = lax.broadcasted_iota(jnp.int32, (n, spare), 0) >= length
    first_column = lax.broadcasted_iota(jnp.int32, (n, spare), 1) == 0
    k_ref[:, :width] = k
    k_ref[:, width:] = jnp.where(first_column & dead, MASKED, 0.0).astype(BF16)
    qa_ref[:, :width] = q
    qa_ref[:, width:] = jnp.where(first_column, 1.0, 0.0).astype(BF16)

    serve(1)
    def scores(h, b):
        first, last = b * step, (b + 1) * step
        q = qa_ref[first:last, :]
        lane = lax.broadcasted_iota(jnp.int32, (1, q.shape[1]), 1)
        keep = head_mask((1, q.shape[1]), h) | (lane >= width)
        return dot_nt(k_ref[:last, :], jnp.where(keep, q, jnp.zeros((), BF16)))

    def attend(h, b, s):
        first, last = b * step, (b + 1) * step
        key = lax.broadcasted_iota(jnp.int32, (step, step), 0)
        query = lax.broadcasted_iota(jnp.int32, (step, step), 1)
        near = jnp.where(key <= query, s[first:], MASKED)
        top = jnp.max(near, 0, keepdims=True)
        if b:
            far = s[:first]
            top = jnp.maximum(top, jnp.max(far, 0, keepdims=True))
        e_near = jnp.exp((near - top).astype(BF16))
        p_ref[0, h, b, first:last, :] = e_near
        o = dot_nn(vt_ref[h, :, first:last], e_near)
        if b:
            e_far = jnp.exp((far - top).astype(BF16))
            p_ref[0, h, b, :first, :] = e_far
            o += dot_nn(vt_ref[h, :, :first], e_far)
        scale = 1.0 / o[HEAD_DIM : HEAD_DIM + 1]
        scale_ref[0, h : h + 1, first:last] = scale
        ot_ref[h * HEAD_DIM : (h + 1) * HEAD_DIM, first:last] = (
            o[:HEAD_DIM] * scale
        ).astype(BF16)

    scale_ref[0, heads:, :] = jnp.zeros((scale_ref.shape[1] - heads, n), F32)
    ready = [scores(h, 0) for h in range(heads)]
    for b in range(n // step):
        ahead = [scores(h, b + 1) for h in range(heads)] if b + 1 < n // step else None
        for h in range(heads):
            attend(h, b, ready[h])
        ready = ahead
    serve(2)

    gw_ref[0] = allw_ref[t].reshape(gw_ref.shape[1:])
    o = ot_ref[...].T
    o_ref[0] = o
    h1_ref[...] += dot_nt(o, gw_ref[0])

    @pl.when(t == 3)
    def _():
        for i, rows in enumerate(blocks(n, step)):
            xhat, _ = norm_parts(h1_ref[rows, :])
            a2 = (xhat * rows_ref[1:2, :] + rows_ref[6:7, :]).astype(BF16)
            a2_ref[rows, :] = a2
            a2t_ref[:, rows] = a2.T
            for put in puts[i]:
                put.start()
        put_a2t.start()
        recv(seg2.core)
        flush[1][1].start()
        recv(seg1.core)
        flush[0][1].start()
        pass_second(seg1)
        flush[0][2].start()
        links.sent()
        for copies in flush + puts + [[put_a1t, put_a2t]]:
            for copy in copies:
                copy.wait()


N_GATHER = 10 + 13 + 10 + 10 + 10
VMEM_WHOLE = pl.BlockSpec(memory_space=pltpu.VMEM)
ANY_WHOLE = pl.BlockSpec(memory_space=pl.ANY)


def run_fused_forward(tie, lengths, tokens, gains, biases, w_in, w_out, w_expand, w_project):
    groups, n, _ = tokens.shape
    depth, width = w_in.shape[-2:]
    heads = width // HEAD_DIM
    hidden = w_expand.shape[-1]
    w_project = w_project.transpose(0, 2, 1)
    biases = biases.transpose(1, 0, 2)
    own = gains.shape[-1]
    return pl.pallas_call(
        fused_forward,
        grid=(groups,),
        in_specs=[SMEM_WHOLE, SMEM_WHOLE, ANY_WHOLE] + [VMEM_WHOLE] * 6,
        out_specs=[
            group(D, 3 * width), group(D, width), ANY_WHOLE, ANY_WHOLE, VMEM_WHOLE,
            group(n, width), group(n, width), group(width, n), group(heads, n // 256, n, 256),
            group(8, n), group(n, width), ANY_WHOLE, ANY_WHOLE, ANY_WHOLE, ANY_WHOLE,
        ],
        out_shape=[
            shaped(BF16, groups, D, 3 * width), shaped(BF16, groups, D, width),
            shaped(BF16, groups, Z_DEV, Y_DEV, depth, hidden),
            shaped(BF16, groups, Z_DEV, Y_DEV, depth, hidden),
            shaped(F32, 16, D),
            shaped(BF16, groups, n, width), shaped(BF16, groups, n, width),
            shaped(BF16, groups, width, n), shaped(BF16, groups, heads, n // 256, n, 256),
            shaped(F32, groups, 8, n), shaped(BF16, groups, n, width), shaped(BF16, D, n), shaped(F32, n, D),
            shaped(BF16, n, D), shaped(BF16, D, n),
        ],
        scratch_shapes=[
            pltpu.VMEM((depth, 3 * width), BF16), pltpu.VMEM((depth, width), BF16),
            pltpu.VMEM((depth, hidden), BF16), pltpu.VMEM((depth, hidden), BF16),
            pltpu.VMEM((128, 128), F32), pltpu.VMEM((own, 128), F32),
            pltpu.VMEM((groups, Z_DEV, Y_DEV, depth, 3 * width), BF16),
            pltpu.VMEM((groups, Z_DEV, Y_DEV, depth, width), BF16),
            pltpu.VMEM((groups, Z_DEV, Y_DEV, depth, hidden), BF16),
            pltpu.VMEM((groups, Z_DEV, Y_DEV, depth, hidden), BF16),
            pltpu.VMEM((Z_DEV, Y_DEV, X_DEV, C_DEV, own, 128), F32),
            pltpu.VMEM((groups, 8, 3 * width), F32),
            pltpu.VMEM((n, D), BF16), pltpu.VMEM((n, D), BF16), pltpu.VMEM((n, 256), BF16),
            pltpu.VMEM((n, 256), BF16), pltpu.VMEM((heads, HEAD_DIM + 16, n), BF16),
            pltpu.VMEM((width, n), BF16),
            pltpu.VMEM((D, n), BF16), pltpu.VMEM((n, D), F32), pltpu.VMEM((n, D), BF16),
            pltpu.VMEM((D, n), BF16),
            pltpu.SemaphoreType.DMA((N_GATHER,)), pltpu.SemaphoreType.DMA((N_GATHER,)),
            pltpu.SemaphoreType.DMA((3,)), pltpu.SemaphoreType.DMA((2, 4)),
            pltpu.SemaphoreType.DMA((2, n // 256)),
        ],
        compiler_params=pltpu.CompilerParams(
            vmem_limit_bytes=VMEM_LIMIT, collective_id=0, has_side_effects=True
        ),
        name="fused_forward",
    )(tie, lengths, tokens, gains, biases, w_in, w_out, w_expand, w_project)


class Result:
    def __init__(self, links, place, own_ref, passing_ref, out_ref, step, sem, count):
        self.x, self.core, self.far, self.keep, self.keep_far = [], [], [], [], []
        for i in range(count):
            rows = pl.ds(i * step, step)
            mine, theirs = out_ref.at[place.t, rows], out_ref.at[place.ts[2], rows]
            own, passing = own_ref.at[rows], passing_ref.at[rows]
            self.x.append(links.add(place.to_x, own, passing, 4))
            self.core.append(links.add(place.to_core, own, mine, 4))
            self.far.append(links.add(place.to_core, passing, theirs, 4))
            self.keep.append(pltpu.make_async_copy(own, mine, sem.at[0, i]))
            self.keep_far.append(pltpu.make_async_copy(passing, theirs, sem.at[1, i]))

    def send(self, i):
        start(self.x[i], self.core[i], self.keep[i])

    def pass_on(self, i):
        recv(self.x[i])
        start(self.far[i], self.keep_far[i])

    def finish(self):
        recv(self.core, self.far)
        for copy in self.keep + self.keep_far:
            copy.wait()


def low(value):
    return jnp.asarray(value, BF16)


def pair_order(i):
    return i + 1 - 2 * (i % 2)


def fused_feed_forward(
    len_ref, cot_ref, a2_ref, a2t_in, h1_in, far1_ref, far2_ref, rows_ref,
    out_out, fold_ref, work_out, dh1_out, gb_out, gbt_out, sums_ref,
    gf_ref, gft_ref, feed_ref, da2_ref, h_ref, df_ref, weights_ref, missing_ref, third_ref,
    stage_ref, land_ref, near_ref, cross_ref, a2t_ref, h1_ref, out_ref, work_ref,
    send_sem, recv_sem, local_sem, row_sem,
):
    t = pl.program_id(0)
    n = gf_ref.shape[0]
    step = 256
    depth = stage_ref.shape[-2]
    place = Place()
    length = len_ref[place.t]
    links = Links(send_sem, recv_sem)
    y, other = place.y, place.other_y
    last = [
        links.add(place.to_x, far1_ref.at[0, :, other], missing_ref.at[0, 0], Z_DEV),
        links.add(place.to_y, far2_ref.at[2, :, y], missing_ref.at[1, 0], Z_DEV),
    ]
    last_core = [
        links.add(place.to_core, missing_ref.at[i, 0], missing_ref.at[i, 1], Z_DEV)
        for i in range(2)
    ]
    third = [
        links.add(place.to_core, far_ref.at[2, :, y], third_ref.at[i], Z_DEV)
        for i, far_ref in enumerate([far1_ref, far2_ref])
    ]
    core = [
        [
            links.add(place.to_core, stage_ref.at[i], land_ref.at[s, i], Z_DEV) for i in range(2)
        ]
        for s in range(2)
    ]
    cross = [
        links.add(place.to_y, near_ref.at[i, :, other], cross_ref.at[i], Z_DEV)
        for i in range(2)
    ]
    fetch = pltpu.make_async_copy(cot_ref.at[place.t], gf_ref, local_sem.at[0])
    gb_ref, gbt_ref, dh1_ref = gf_ref, gft_ref, da2_ref
    late = [
        pltpu.make_async_copy(a2t_in, a2t_ref, local_sem.at[5]),
        pltpu.make_async_copy(h1_in, h1_ref, local_sem.at[6]),
    ]
    puts = []
    for i in range(n // step):
        rows = pl.ds(i * step, step)
        puts.append([
            pltpu.make_async_copy(ref.at[rows], out.at[rows], row_sem.at[j, i])
            for j, (ref, out) in enumerate(
                [(out_ref, out_out), (dh1_ref, dh1_out), (gb_ref, gb_out)]
            )
        ])
    put_gbt = pltpu.make_async_copy(gbt_ref, gbt_out, local_sem.at[7])
    put_work = pltpu.make_async_copy(work_ref, work_out, local_sem.at[8])
    k = pair_order(t)
    mine = place.group(k)

    def load(step, whole, slot):
        for i, far_ref in enumerate([far1_ref, far2_ref]):
            group = far_ref.at[pair_order(step)]
            to = weights_ref.at[slot, i]
            if not whole:
                group, to = group.at[:, y], to.at[:, y]
            yield pltpu.make_async_copy(group, to, local_sem.at[1 + 2 * slot + i])

    def live_rows(b):
        at = b * step + lax.broadcasted_iota(jnp.int32, (step, 1), 0)
        return (at < length).astype(F32)

    @pl.when(t == 0)
    def _():
        fetch.start()
        for copy in load(0, True, 0):
            copy.start()
        for copy in late:
            copy.start()
        place.greet()
        start(last, third)
        sums_ref[...] = jnp.zeros_like(sums_ref)
        feed_ref[...] = jnp.zeros_like(feed_ref)
        da2_ref[...] = jnp.zeros_like(da2_ref)
        fetch.wait()

        @pl.loop(0, n // step)
        def _(b):
            rows = pl.ds(pl.multiple_of(b * step, step), step)
            g = (gf_ref[rows, :].astype(F32) * live_rows(b)).astype(BF16)
            gf_ref[rows, :] = g
            gft_ref[:, rows] = g.T
            sums_ref[7:8, :] += jnp.sum(g.astype(F32), 0, keepdims=True)

    for i in range(4):
        @pl.when(t == i)
        def _():
            if i == 2:
                recv(last_core, third)
            else:
                for copy in load(i, i < 2, i % 2):
                    copy.wait()
            if i in (0, 2):
                for copy in load(i + 1, i + 1 < 2, (i + 1) % 2):
                    copy.start()
            for j in range(2):
                if i == 2:
                    weights_ref[0, j, :, y] = third_ref[j]
                if i >= 2:
                    weights_ref[i % 2, j, :, other] = missing_ref[j, 3 - i]

    bias = rows_ref[pl.ds(8 + mine, 1), :]
    w1 = weights_ref[t % 2, 0].reshape(D, -1)
    w2 = weights_ref[t % 2, 1].reshape(D, -1)
    column = jnp.zeros((1, w1.shape[1]), F32)
    for rows in blocks(n, step):
        f = (dot_nn(a2_ref[rows, :], w1) + bias).astype(BF16)
        dh = dot_nn(gf_ref[rows, :], w2)
        f2 = f * f
        th = jnp.tanh(f * (low(SQRT_2_PI) + low(SQRT_2_PI * 0.044715) * f2))
        half = low(0.5) + low(0.5) * th
        h = f * half
        slope = half + f * (low(0.5) - low(0.5) * th * th) * (
            low(SQRT_2_PI) + low(3 * SQRT_2_PI * 0.044715) * f2
        )
        df = (dh * slope.astype(F32)).astype(BF16)
        h_ref[rows, :] = h
        df_ref[rows, :] = df
        column += jnp.sum(df.astype(F32), 0, keepdims=True)
        feed_ref[rows, :] += dot_nt(h, w2)
        da2_ref[rows, :] += dot_nt(df, w1)
    sums_ref[pl.ds(8 + mine, 1), :] = column

    @pl.when(t == 1)
    def _():
        recv(last)
        start(last_core)

    @pl.when(t == 0)
    def _():
        late[0].wait()

    def weight_grad(left_ref, right_ref):
        value = dot_nn(left_ref[...], right_ref[...])
        return value.reshape(Z_DEV, Y_DEV, depth, value.shape[-1]).astype(BF16)

    grad1 = weight_grad(a2t_ref, df_ref)
    grad2 = weight_grad(gft_ref, h_ref)

    def put(ref):
        ref[0] = grad1
        ref[1] = grad2

    def reduced(ref):
        return lambda i, s, z: (
            ref[i, z].astype(F32) + land_ref[s, i, z].astype(F32)
        ).astype(BF16)

    @pl.when(t == 0)
    def _():
        put(stage_ref)
        start(core[0])

    @pl.when(t == 1)
    def _():
        put(near_ref)
        recv(core[0])

        @pl.loop(0, Z_DEV)
        def _(z):
            for i in range(2):
                near_ref[i, z] = reduced(near_ref)(i, 0, z)

        start(cross)

    @pl.when(t == 2)
    def _():
        for copy in core[0]:
            copy.wait_send()
        put(stage_ref)
        start(core[1])

    @pl.when(t == 3)
    def _():
        put(work_ref)
        late[1].wait()
        for i, rows in enumerate(blocks(n, step)):
            live = live_rows(i)
            h1 = h1_ref[rows, :]
            out_ref[rows, :] = (live * (h1 + (feed_ref[rows, :] + rows_ref[7:8, :]))).astype(BF16)
            xhat, r = norm_parts(h1)
            da2 = da2_ref[rows, :]
            sums_ref[1:2, :] += jnp.sum(da2 * xhat, 0, keepdims=True)
            sums_ref[6:7, :] += jnp.sum(da2, 0, keepdims=True)
            dg = da2 * rows_ref[1:2, :]
            dv = r * (
                dg
                - jnp.mean(dg, -1, keepdims=True)
                - xhat * jnp.mean(dg * xhat, -1, keepdims=True)
            )
            dh1 = gf_ref[rows, :].astype(F32) + dv
            dh1_ref[rows, :] = dh1
            gb = dh1.astype(BF16)
            gb_ref[rows, :] = gb
            gbt_ref[:, rows] = gb.T
            sums_ref[5:6, :] += jnp.sum(gb.astype(F32), 0, keepdims=True)
            for copy in puts[i]:
                copy.start()
        put_gbt.start()
        recv(core[1])

        @pl.loop(0, Z_DEV)
        def _(z):
            for i in range(2):
                work_ref[i, z] = reduced(work_ref)(i, 1, z)

        put_work.start()
        recv(cross)

        @pl.loop(0, Z_DEV)
        def _(z):
            for i in range(2):
                fold_ref[i, z] = (
                    near_ref[i, z, y].astype(F32) + cross_ref[i, z].astype(F32)
                ).astype(BF16)

        links.sent(*core[0])
        for copies in puts + [[put_gbt, put_work]]:
            for copy in copies:
                copy.wait()


def run_fused_feed_forward(lengths, cot, a2, a2t, h1, g1, g2, rows):
    n = cot.shape[1]
    groups, _, _, depth, hidden = g1.shape
    both = (2, Z_DEV, Y_DEV, depth, hidden)
    fold = (2, Z_DEV, depth, hidden)
    return pl.pallas_call(
        fused_feed_forward,
        grid=(groups,),
        in_specs=[SMEM_WHOLE, ANY_WHOLE, VMEM_WHOLE] + [ANY_WHOLE] * 4 + [VMEM_WHOLE],
        out_specs=[ANY_WHOLE, VMEM_WHOLE] + [ANY_WHOLE] * 4 + [VMEM_WHOLE],
        out_shape=[
            shaped(BF16, n, D), shaped(BF16, *fold), shaped(BF16, *both), shaped(F32, n, D),
            shaped(BF16, n, D), shaped(BF16, D, n), shaped(F32, 16, D),
        ],
        scratch_shapes=[
            pltpu.VMEM((n, D), BF16), pltpu.VMEM((D, n), BF16), pltpu.VMEM((n, D), F32),
            pltpu.VMEM((n, D), F32), pltpu.VMEM((n, hidden), BF16), pltpu.VMEM((n, hidden), BF16),
            pltpu.VMEM((2,) + both, BF16),
            pltpu.VMEM((2,) + fold, BF16), pltpu.VMEM(fold, BF16), pltpu.VMEM(both, BF16),
            pltpu.VMEM((2,) + both, BF16),
            pltpu.VMEM(both, BF16), pltpu.VMEM(fold, BF16),
            pltpu.VMEM((D, n), BF16), pltpu.VMEM((n, D), F32), pltpu.VMEM((n, D), BF16),
            pltpu.VMEM(both, BF16),
            pltpu.SemaphoreType.DMA((12,)), pltpu.SemaphoreType.DMA((12,)),
            pltpu.SemaphoreType.DMA((9,)), pltpu.SemaphoreType.DMA((3, n // 256)),
        ],
        compiler_params=pltpu.CompilerParams(
            vmem_limit_bytes=VMEM_LIMIT, collective_id=1, has_side_effects=True
        ),
        name="fused_feed_forward",
    )(lengths, cot, a2, a2t, h1, g1, g2, rows)
class Reduce:
    def __init__(
        self, links, place, work, acc, cross_ref, far_ref, mid_ref, last_ref, side_ref,
        slots=(0, 1),
    ):
        self.place, self.work, self.acc = place, work, acc
        self.cross_ref, self.far_ref, self.mid_ref = cross_ref, far_ref, mid_ref
        self.last_ref, self.side_ref = last_ref, side_ref
        zs = place.zs
        self.y = {
            s: [
                links.add(
                    place.to_y, work(s, zs[j], place.other_y), cross_ref.at[s, zs[j]], 2
                )
                for j in (1, 3, 2, 0)
            ]
            for s in slots
        }
        self.z = [
            [
                links.add(place.to_z[1], acc(s, zs[1]), far_ref.at[s, 0], 2),
                links.add(place.to_z[1], acc(s, zs[3]), far_ref.at[s, 1], 2),
                links.add(place.to_z[2], mid_ref.at[s, 1], far_ref.at[s, 2], 2),
            ]
            for s in range(2)
        ]
        self.x = links.add(place.to_x, last_ref, side_ref, 2)

    def fold_y(self, s, half):
        for i, j in [(0, 1), (1, 3), (2, 2), (3, 0)][2 * half : 2 * half + 2]:
            z = self.place.zs[j]
            recv(self.y[s][i])
            value = self.work(s, z, self.place.y)[...].astype(F32)
            self.acc(s, z)[...] = (value + self.cross_ref[s, z].astype(F32)).astype(BF16)
            if i < 2:
                start(self.z[s][i])

    def fold_z(self, s):
        recv(self.z[s][:2])
        for i in (1, 0):
            value = self.acc(s, self.place.zs[2 * i])[...].astype(F32)
            self.mid_ref[s, i] = (value + self.far_ref[s, i].astype(F32)).astype(BF16)
            if i:
                start(self.z[s][2])

    def own(self, s):
        recv(self.z[s][2])
        return self.mid_ref[s, 0].astype(F32) + self.far_ref[s, 2].astype(F32)

    def send_x(self):
        self.last_ref[...] = self.own(1).astype(BF16)
        start(self.x)

    def total(self):
        value = self.own(0)
        recv(self.x)
        return value + self.side_ref[...].astype(F32)


def fused_backward(
    tokens_ref, gq_in, gw_in, rows_ref, dh1_ref, gb_ref, gbt_in, q_in, v_in, kt_in,
    p_ref, scale_in, o_in, a1t_in, layer_in, fold_in, work_in, early_ref,
    out_ref, layerout_ref, part0_ref, partw_ref, part1_ref, part2_ref, total_ref,
    gq_ref, gw_ref, q_ref, v_ref, kt_ref, scale_ref, o_ref,
    a1t_ref, gbt_ref, layer_ref, fold_ref, work_ref, do_ref, delta_ref, dkv_ref, dqkv_ref, da1_ref, own_ref, passing_ref, passlayer_ref, bqv_ref,
    folded_ref, cross1_ref, far1_ref, mid1_ref, last1_ref, side1_ref,
    cross2_ref, far2_ref, mid2_ref, last2_ref, side2_ref,
    stagew_ref, landw_ref, workw_ref, crossw_ref, farw_ref, midw_ref, lastw_ref, sidew_ref,
    stage0_ref, land0_ref, work0_ref, cross0_ref, far0_ref, mid0_ref, last0_ref, side0_ref,
    sums_ref, sumland_ref,
    send_sem, recv_sem, local_sem, result_sem, group_sem,
):
    t = pl.program_id(0)
    n = own_ref.shape[0]
    width = gw_ref.shape[-1]
    depth = part0_ref.shape[0]
    heads = width // HEAD_DIM
    step = n // 4
    place = Place()
    y = place.y
    links = Links(send_sem, recv_sem)
    k, i = group_and_block(t)
    mine = place.group(k)
    now = k % 2
    out = Result(links, place, own_ref, passing_ref, out_ref, step, result_sem.at[0], 4)
    layer = Result(links, place, layer_ref, passlayer_ref, layerout_ref, step, result_sem.at[1], 4)
    fetch = pltpu.make_async_copy(tokens_ref.at[place.t], own_ref, local_sem.at[0])
    fetch_layer, fetch_work, fetch_fold, fetch_gbt, fetch_a1t = [
        pltpu.make_async_copy(there, here, local_sem.at[1 + j])
        for j, (there, here) in enumerate([
            (layer_in, layer_ref), (work_in, work_ref), (fold_in, fold_ref),
            (gbt_in, gbt_ref), (a1t_in, a1t_ref),
        ])
    ]
    def operands(group):
        slot = group % 2
        pairs = [
            (gw_in, gw_ref), (scale_in, scale_ref), (o_in, o_ref), (v_in, v_ref),
            (q_in, q_ref), (kt_in, kt_ref), (gq_in, gq_ref),
        ]
        return [
            pltpu.make_async_copy(there.at[group], here.at[slot], group_sem.at[slot, j])
            for j, (there, here) in enumerate(pairs)
        ]

    corew = [links.add(place.to_core, stagew_ref, landw_ref.at[i], Z_DEV) for i in range(2)]
    core0 = [links.add(place.to_core, stage0_ref, land0_ref.at[i], Z_DEV) for i in range(2)]
    def half_done(i, *landing):
        return Reduce(
            links, place, lambda s, z, y: work_ref.at[i, z, y],
            lambda s, z: folded_ref.at[i, z] if s else fold_ref.at[i, z],
            *landing, slots=(1,),
        )

    seg1 = half_done(0, cross1_ref, far1_ref, mid1_ref, last1_ref, side1_ref)
    seg2 = half_done(1, cross2_ref, far2_ref, mid2_ref, last2_ref, side2_ref)
    segw = Reduce(
        links, place, lambda s, z, y: workw_ref.at[s, z, y],
        lambda s, z: workw_ref.at[s, z, y],
        crossw_ref, farw_ref, midw_ref, lastw_ref, sidew_ref,
    )
    seg0 = Reduce(
        links, place, lambda s, z, y: work0_ref.at[s, z, y],
        lambda s, z: work0_ref.at[s, z, y],
        cross0_ref, far0_ref, mid0_ref, last0_ref, side0_ref,
    )
    sum_core, sum_y, *sum_z, sum_x = [
        links.add(to, sums_ref.at[i], sumland_ref.at[j])
        for j, (i, to) in enumerate(
            zip([0, 1, 2, 2, 2, 3], [place.to_core, place.to_y] + place.to_z[1:] + [place.to_x])
        )
    ]

    def when(point):
        return pl.when(t == point)

    @when(0)
    def _():
        start(fetch_layer, operands(1), fetch_work, fetch_fold, fetch_gbt, operands(0))
        start(fetch, fetch_a1t)
        place.greet()
        fetch_layer.wait()
        for i in range(4):
            layer.send(i)
        fetch_work.wait()
        start(seg1.y[1], seg2.y[1])
        fetch_fold.wait()
        start(seg1.z[0][:2], seg2.z[0][:2])
        bqv_ref[...] = jnp.zeros_like(bqv_ref)
        sums_ref[0] = early_ref[...]
        fetch_gbt.wait()

    def add_core():
        recv(corew[1])

        @pl.loop(0, Z_DEV)
        def _(z):
            workw_ref[1, z] = (
                workw_ref[1, z].astype(F32) + landw_ref[1, z].astype(F32)
            ).astype(BF16)

        start(segw.y[1])

    def wait(copies):
        for copy in copies:
            copy.wait()

    @when(0)
    def _():
        wait(operands(1))

    @when(4)
    def _():
        start(operands(3))
        wait(operands(0))

    @when(8)
    def _():
        start(operands(2))
        wait(operands(3))

    @when(9)
    def _():
        wait(operands(2))

    plan = [
        (2, 1, lambda: (seg1.fold_y(1, 0), seg1.fold_z(0))),
        (3, 1, lambda: layer.pass_on(0)),
        (4, 0, lambda: (seg1.fold_y(1, 1), seg2.fold_z(0))),
        (4, 1, lambda: layer.pass_on(1)),
        (5, 1, lambda: (seg1.fold_z(1), seg2.fold_y(1, 0))),
        (8, 0, lambda: (seg2.fold_y(1, 1), layer.pass_on(2))),
        (8, 1, lambda: (seg1.send_x(), segw.fold_y(0, 0), segw.fold_y(0, 1))),
        (9, 0, add_core),
        (9, 1, lambda: (seg2.fold_z(1), seg0.fold_y(0, 0), layer.pass_on(3))),
        (10, 1, lambda: segw.fold_z(0)),
        (11, 1, lambda: (seg2.send_x(), seg0.fold_y(0, 1))),
        (12, 1, lambda: (segw.fold_y(1, 0), segw.fold_y(1, 1))),
        (13, 1, lambda: (seg0.fold_z(0), out.pass_on(3))),
        (14, 1, lambda: segw.fold_z(1)),
    ]

    def serve(point):
        for at, where, act in plan:
            if where == point:
                pl.when(t == at)(lambda act=act: (act(), None)[1])

    @pl.when((t == 0) | (t == 4) | (t == 8) | (t == 9))
    def _():
        pick = (
            lax.broadcasted_iota(jnp.int32, (8, width), 1) // HEAD_DIM
            == lax.broadcasted_iota(jnp.int32, (8, width), 0)
        ).astype(BF16)

        @pl.loop(0, n // step)
        def _(i):
            rows = pl.ds(pl.multiple_of(i * step, step), step)
            columns = scale_ref[now, :, rows].T
            lane = lax.broadcasted_iota(jnp.int32, (step, width), 1)
            scale = columns[:, heads - 1 : heads]
            for h in reversed(range(heads - 1)):
                scale = jnp.where(lane < (h + 1) * HEAD_DIM, columns[:, h : h + 1], scale)
            do = (dot_nn(gb_ref[rows, :], gw_ref[now]) * scale).astype(BF16)
            do_ref[now, rows, :] = do
            product = do.astype(F32) * o_ref[now, rows, :].astype(F32)
            high = product.astype(BF16)
            low = (product - high.astype(F32)).astype(BF16)
            delta_ref[now, :, rows] = dot_nt(pick, high) + dot_nt(pick, low)

        value = dot_nn(gbt_ref[...], o_ref[now]).reshape(Z_DEV, Y_DEV, depth, width)
        for s in range(2):
            @when(8 * s)
            def _():
                if s:
                    corew[0].wait_send()
                stagew_ref[...] = value.astype(BF16)
                start(corew[s])

        @when(4)
        def _():
            recv(corew[0])
            workw_ref[0] = (value + landw_ref[0].astype(F32)).astype(BF16)
            start(segw.y[0])

        @when(9)
        def _():
            workw_ref[1] = value.astype(BF16)

    serve(0)

    for ii in reversed(range(4)):
        @pl.when(i == ii)
        def _():
            first, last = ii * step, (ii + 1) * step
            do = do_ref[now, first:last, :]
            q = q_ref[now, first:last, :]
            v = v_ref[now, :last, :]
            lane = lax.broadcasted_iota(jnp.int32, (1, width), 1)
            dk, dv, dq = None, None, []
            for h in range(heads):
                low, high = h * HEAD_DIM, (h + 1) * HEAD_DIM
                here = (lane >= low) & (lane < high)
                p = p_ref[0, h, 0, :last, :]
                dp = dot_nt(v, jnp.where(here, do, jnp.zeros((), BF16)))
                ds = p * (dp - delta_ref[now, h : h + 1, first:last]).astype(BF16)
                part = dot_nn(p, do)
                dv = part if dv is None else jnp.where(lane < low, dv, part)
                part = dot_nn(ds, q)
                dk = part if dk is None else jnp.where(lane < low, dk, part)
                dq.append(dot_nn(kt_ref[now, low:high, :last], ds))
            if ii == 3:
                dkv_ref[now, 0] = dk
                dkv_ref[now, 1] = dv
            else:
                dkv_ref[now, 0, :last, :] += dk
                dkv_ref[now, 1, :last, :] += dv
            dk = dkv_ref[now, 0, first:last, :].astype(BF16)
            dv = dkv_ref[now, 1, first:last, :].astype(BF16)
            dq = (jnp.concatenate(dq, 0) * HEAD_DIM ** -0.5).astype(BF16).T
            dqkv_ref[now, first:last, :width] = dq
            dqkv_ref[now, first:last, width : 2 * width] = dk
            dqkv_ref[now, first:last, 2 * width :] = dv
            bqv_ref[mine, 0:1, :] += jnp.sum(dq.astype(F32), 0, keepdims=True)
            bqv_ref[mine, 1:2, :] += jnp.sum(dv.astype(F32), 0, keepdims=True)

            @pl.when(t >= 8)
            def _():
                da1_ref[first:last, :] += dot_nt(dqkv_ref[now, first:last, :], gq_ref[now])

    serve(1)

    @pl.when((t > 8) & (t % 2 == 1))
    def _():
        rows = pl.ds(pl.multiple_of(i * step, step), step)
        xhat, r = norm_parts(own_ref[rows, :].astype(F32))
        da1 = da1_ref[rows, :]
        sums_ref[0, 0:1, :] += jnp.sum(da1 * xhat, 0, keepdims=True)
        sums_ref[0, 2:3, :] += jnp.sum(da1, 0, keepdims=True)
        dg = da1 * rows_ref[0:1, :]
        dv = r * (
            dg
            - jnp.mean(dg, -1, keepdims=True)
            - xhat * jnp.mean(dg * xhat, -1, keepdims=True)
        )
        own_ref[rows, :] = (dh1_ref[...] + dv).astype(BF16)
        for ii in range(4):
            @pl.when(i == ii)
            def _():
                out.send(ii)

    @pl.when((t == 3) | (t == 7) | (t > 13))
    def _():
        @when(3)
        def _():
            fetch.wait()
            fetch_a1t.wait()

        @when(3)
        def _():
            da1_ref[...] = dot_nt(dqkv_ref[now], gq_ref[now])

        @when(7)
        def _():
            da1_ref[...] += dot_nt(dqkv_ref[now], gq_ref[now])

        value = dot_nn(a1t_ref[...], dqkv_ref[now]).reshape(Z_DEV, Y_DEV, depth, 3 * width)
        for s in range(2):
            @when(3 + 11 * s)
            def _():
                if s:
                    core0[0].wait_send()
                stage0_ref[...] = value.astype(BF16)
                start(core0[s])

            @when(7 + 8 * s)
            def _():
                recv(core0[s])
                work0_ref[s] = (value + land0_ref[s].astype(F32)).astype(BF16)
                start(seg0.y[s])

    @when(15)
    def _():
        for s in range(4):
            sums_ref[0, 3:5, s * width : (s + 1) * width] = bqv_ref[s, 0:2, :]
        start(sum_core)
        segw.send_x()
        out.pass_on(2)
        recv(sum_core)
        sums_ref[1] = sums_ref[0] + sumland_ref[0]
        start(sum_y)
        seg0.fold_y(1, 0)
        out.pass_on(1)
        seg0.fold_y(1, 1)
        recv(sum_y)
        sums_ref[2] = sums_ref[1] + sumland_ref[1]
        start(sum_z)
        seg0.fold_z(1)
        recv(sum_z)
        sums_ref[3] = (sums_ref[2] + sumland_ref[2]) + (sumland_ref[3] + sumland_ref[4])
        start(sum_x)
        part1_ref[...] = seg1.total()
        part2_ref[...] = seg2.total()
        seg0.send_x()
        partw_ref[...] = segw.total()
        layer.finish()
        out.pass_on(0)
        recv(sum_x)
        total_ref[...] = sums_ref[3] + sumland_ref[5]
        part0_ref[...] = seg0.total()
        out.finish()
        links.sent(corew[0], core0[0])


def group_and_block(t):
    early = t < 8
    return (
        jnp.where(early, 1 - t // 4, 3 - t % 2),
        3 - jnp.where(early, t % 4, jnp.maximum(t - 8, 0) // 2),
    )


def run_fused_backward(
    tokens, gq, gw, rows, dh1, gb, gbt, q, v, kt, p, scale, o, a1t, layer, fold, work, early
):
    groups, n, _ = tokens.shape
    width = gw.shape[-1]
    heads = width // HEAD_DIM
    hidden = fold.shape[-1]
    depth = D // (Z_DEV * Y_DEV)
    step = n // 4

    p_spec = pl.BlockSpec(
        (1, heads, 1, n, step),
        lambda t: (group_and_block(t)[0], 0, group_and_block(t)[1], 0, 0),
    )

    copies = 2 * 12 + 4 + 2 * 15 + 2 * 11 + 6

    def landing(lanes):
        return [
            pltpu.VMEM((2, Z_DEV, depth, lanes), BF16),
            pltpu.VMEM((2, 3, depth, lanes), BF16), pltpu.VMEM((2, 2, depth, lanes), BF16),
            pltpu.VMEM((depth, lanes), BF16), pltpu.VMEM((depth, lanes), BF16),
        ]

    def working(lanes):
        block = (Z_DEV, Y_DEV, depth, lanes)
        return [pltpu.VMEM(block, BF16)] + [pltpu.VMEM((2,) + block, BF16)] * 2

    return pl.pallas_call(
        fused_backward,
        grid=(4 * groups,),
        in_specs=[
            ANY_WHOLE, ANY_WHOLE, ANY_WHOLE, VMEM_WHOLE,
            pl.BlockSpec((step, D), lambda t: (group_and_block(jnp.maximum(t, 8))[1], 0)),
            VMEM_WHOLE, ANY_WHOLE, ANY_WHOLE, ANY_WHOLE, ANY_WHOLE, p_spec,
            ANY_WHOLE, ANY_WHOLE, ANY_WHOLE, ANY_WHOLE, ANY_WHOLE, ANY_WHOLE, VMEM_WHOLE,
        ],
        out_specs=[ANY_WHOLE] * 2 + [VMEM_WHOLE] * 5,
        out_shape=[
            shaped(BF16, groups, n, D), shaped(BF16, groups, n, D),
            shaped(F32, depth, 3 * width),
            shaped(F32, depth, width), shaped(F32, depth, hidden),
            shaped(F32, depth, hidden), shaped(F32, 16, D),
        ],
        scratch_shapes=[
            pltpu.VMEM((2, D, 3 * width), BF16), pltpu.VMEM((2, D, width), BF16),
            pltpu.VMEM((2, n, width), BF16), pltpu.VMEM((2, n, width), BF16),
            pltpu.VMEM((2, width, n), BF16), pltpu.VMEM((2, 8, n), F32),
            pltpu.VMEM((2, n, width), BF16),
            pltpu.VMEM((D, n), BF16), pltpu.VMEM((D, n), BF16), pltpu.VMEM((n, D), BF16),
            pltpu.VMEM((2, Z_DEV, depth, hidden), BF16),
            pltpu.VMEM((2, Z_DEV, Y_DEV, depth, hidden), BF16),
            pltpu.VMEM((2, n, width), BF16),
            pltpu.VMEM((2, 8, n), F32), pltpu.VMEM((2, 2, n, width), F32),
            pltpu.VMEM((2, n, 3 * width), BF16), pltpu.VMEM((n, D), F32),
            pltpu.VMEM((n, D), BF16), pltpu.VMEM((n, D), BF16), pltpu.VMEM((n, D), BF16),
            pltpu.VMEM((groups, 8, width), F32),
        ]
        + landing(hidden)[:1] + landing(hidden) + landing(hidden)
        + working(width) + landing(width)
        + working(3 * width) + landing(3 * width)
        + [
            pltpu.VMEM((4, 16, D), F32), pltpu.VMEM((6, 16, D), F32),
            pltpu.SemaphoreType.DMA((copies,)), pltpu.SemaphoreType.DMA((copies,)),
            pltpu.SemaphoreType.DMA((6,)), pltpu.SemaphoreType.DMA((2, 2, 4)),
            pltpu.SemaphoreType.DMA((2, 7)),
        ],
        compiler_params=pltpu.CompilerParams(
            vmem_limit_bytes=VMEM_LIMIT, collective_id=2, has_side_effects=True
        ),
        name="fused_backward",
    )(tokens, gq, gw, rows, dh1, gb, gbt, q, v, kt, p, scale, o, a1t, layer, fold, work, early)


def place_gradients(
    tie_ref, sums_ref, part0_ref, partw_ref, part1_ref, part2_ref, near_out_ref,
    near_grad_ref, far_out_ref, far_grad_ref, gains_ref, bias_ref, in_ref, out_ref, expand_ref,
    project_ref,
):
    far_out_ref[...] = near_out_ref[...]
    far_grad_ref[...] = near_grad_ref[...]
    own = gains_ref.shape[-1]
    width = partw_ref.shape[-1]

    @pl.when(pl.program_id(0) == 0)
    def _():
        first = (lax.axis_index("dp") * 4 + lax.axis_index("tensor")) * own
        feature = lax.broadcasted_iota(jnp.int32, (D, 128), 0)
        lane = lax.broadcasted_iota(jnp.int32, (D, 128), 1)
        chosen = ((feature == first + lane) & (lane < own)).astype(F32)
        sums = lax.dot_general(
            sums_ref[...], chosen, (((1,), (0,)), ((), ())),
            precision=lax.Precision.HIGHEST, preferred_element_type=F32,
        )[:, :own]
        s0, s1, s2, s3 = tie_ref[0], tie_ref[1], tie_ref[2], tie_ref[3]
        w_out = partw_ref[...].T

        def at(source, wanted, value):
            return jnp.where(source == wanted, value, jnp.zeros_like(value))

        row = lax.broadcasted_iota(jnp.int32, (NSRC, own), 0)
        for i, wanted in enumerate([s0, s0, s0, s1, s2, s3, s2, s2, s2, s2]):
            bias_ref[i] = jnp.where(row == wanted, sums[2 + i : 3 + i], 0.0)
        for s in range(NSRC):
            gains_ref[s, 0:1] = at(s, s0, sums[0:1])
            gains_ref[s, 1:2] = at(s, s2, sums[1:2])
            for j in range(3):
                in_ref[s, j] = at(s, s0, part0_ref[:, j * width : (j + 1) * width])
            out_ref[s] = at(s, s1, w_out)
            expand_ref[s] = at(s, s2, part1_ref[...])
            project_ref[s] = at(s, s3, part2_ref[...])


def run_place_gradients(tie, sums, part0, partw, part1, part2, out, grad, like):
    slots, n, _ = grad.shape
    gains, biases, w_in, w_out, w_expand, w_project = [item.shape for item in like]
    shapes = [
        gains, (biases[1], biases[0], biases[2]), w_in, w_out, w_expand,
        (w_project[0], w_project[2], w_project[1]),
    ]
    out, grad, gains, biases, w_in, w_out, w_expand, w_project = pl.pallas_call(
        place_gradients,
        grid=(slots,),
        in_specs=[SMEM_WHOLE] + [VMEM_WHOLE] * 5
        + [group(n, D), group(n, D)],
        out_specs=[group(n, D), group(n, D)] + [VMEM_WHOLE] * 6,
        out_shape=[shaped(BF16, slots, n, D)] * 2 + [shaped(F32, *item) for item in shapes],
        compiler_params=pltpu.CompilerParams(vmem_limit_bytes=VMEM_LIMIT),
        name="place_gradients",
    )(tie, sums, part0, partw, part1, part2, out, grad)
    biases = biases.transpose(1, 0, 2)
    return out, grad, gains, biases, w_in, w_out, w_expand, w_project.transpose(0, 2, 1)


def plain_step(
    tokens, lengths, tie_map, norm_gains, bias_rows, attention_in, attention_out,
    expand_weight, project_weight, cotangent,
):
    slot_rows = tokens.shape[0] // lengths.shape[0]
    me = lax.axis_index("tensor")
    in_local = lax.dynamic_index_in_dim(attention_in, tie_map[0], 0, keepdims=False)
    out_local = lax.dynamic_index_in_dim(attention_out, tie_map[1], 0, keepdims=False)
    expand_local = lax.dynamic_index_in_dim(expand_weight, tie_map[2], 0, keepdims=False)
    project_local = lax.dynamic_index_in_dim(project_weight, tie_map[3], 0, keepdims=False)
    local0 = jnp.concatenate([in_local, out_local.T[None]], 0)
    row_kinds = jnp.array([0, 0, 0, 1, 2, 3] + [2] * (FF // D), dtype=jnp.int32)
    gain_kinds = jnp.array([0, 2], dtype=jnp.int32)
    gain_pick = norm_gains[tie_map[gain_kinds], jnp.arange(2)]
    bias_pick = bias_rows[tie_map[row_kinds], jnp.arange(row_kinds.shape[0])]
    vectors = jnp.concatenate([gain_pick, bias_pick], 0)
    x = lax.dynamic_slice_in_dim(tokens, me * slot_rows, slot_rows, 0)
    cot = lax.dynamic_slice_in_dim(cotangent, me * slot_rows, slot_rows, 0)
    length = lax.dynamic_slice_in_dim(lengths, me, 1, 0)
    rows = lax.all_gather(vectors, ("dp", "tensor"), axis=1, tiled=True).astype(F32)
    rows = jnp.concatenate([rows, jnp.zeros((4, D), F32)], 0)

    def gathered(piece, axis):
        piece = lax.all_gather(piece, "dp", axis=axis, tiled=True)
        return lax.all_gather(piece, "tensor", axis=0)

    g0 = gathered(local0, 1)
    g1 = gathered(expand_local, 0)
    g2 = gathered(project_local.T, 0)
    groups, width = g0.shape[0], g0.shape[-1]
    bqv = rows[3:5].reshape(2, groups, width).transpose(1, 0, 2)
    q, v, kt, p, o, a1t, h1, a2, a2t = run_attention_forward(length, x, g0, rows, bqv)
    out, d1, d2, dh1, gb, gbt, sums = run_feed_forward(length, cot, a2, a2t, h1, g1, g2, rows)
    d0, xg, sums_in, sums_qv = run_attention_backward(
        x, g0, rows, dh1, gb, gbt, q, v, kt, p, o, a1t
    )
    layer_out = lax.all_gather(out, "tensor", axis=0, tiled=True)
    tokens_grad = lax.all_gather(xg, "tensor", axis=0, tiled=True)

    def scattered(piece, axis):
        piece = lax.psum_scatter(piece, "tensor", scatter_dimension=0)
        return lax.psum_scatter(piece, "dp", scatter_dimension=axis, tiled=True).astype(F32)

    part0 = scattered(d0, 1)
    part1 = scattered(d1, 0)
    part2 = scattered(d2, 0)
    qv = sums_qv[:, :2].transpose(1, 0, 2).reshape(2, D)
    sums = jnp.concatenate(
        [sums_in[0:1], sums[1:2], sums_in[1:2], qv, sums[5:12]], 0
    )
    sums = lax.psum_scatter(sums, ("dp", "tensor"), scatter_dimension=1, tiled=True)
    return layer_out, tokens_grad, *placed(tie_map, sums, part0, part1, part2)


def fused_step(
    tokens, lengths, tie_map, norm_gains, bias_rows, attention_in, attention_out,
    expand_weight, project_weight, cotangent,
):
    slots = lengths.shape[0]
    tokens = tokens.reshape(slots, -1, D)
    cotangent = cotangent.reshape(slots, -1, D)
    gq, gw, g1, g2, rows, q, v, kt, p, scale, o, a1t, h1, a2, a2t = run_fused_forward(
        tie_map, lengths, tokens, norm_gains, bias_rows, attention_in, attention_out,
        expand_weight, project_weight,
    )
    layer, fold, work, dh1, gb, gbt, early = run_fused_feed_forward(
        lengths, cotangent, a2, a2t, h1, g1, g2, rows
    )
    grad, out, part0, partw, part1, part2, sums = run_fused_backward(
        tokens, gq, gw, rows, dh1, gb, gbt, q, v, kt, p, scale, o, a1t, layer, fold,
        work, early,
    )
    out, grad, *placed_grads = run_place_gradients(
        tie_map, sums, part0, partw, part1, part2, out, grad,
        (norm_gains, bias_rows, attention_in, attention_out, expand_weight, project_weight),
    )
    return out.reshape(-1, D), grad.reshape(-1, D), *placed_grads


def placed(tie_map, sums, part0, part1, part2):
    source = jnp.arange(NSRC, dtype=jnp.int32)

    def place(piece, which):
        pick = (source == tie_map[which]).reshape((NSRC,) + (1,) * piece.ndim)
        return jnp.where(pick, piece[None], 0.0)

    def place_rows(piece, kinds):
        pick = source[:, None] == tie_map[jnp.array(kinds, dtype=jnp.int32)][None, :]
        return jnp.where(pick[:, :, None], piece[None], 0.0)

    return (
        place_rows(sums[:2], [0, 2]),
        place_rows(sums[2:], [0, 0, 0, 1, 2, 3] + [2] * (FF // D)),
        place(part0[:3], 0),
        place(part0[3].T, 1),
        place(part1, 2),
        place(part2.T, 3),
    )


def solution(mesh):
    fused = mesh.shape["dp"] == Z_DEV * Y_DEV and mesh.shape["tensor"] == X_DEV * C_DEV
    return jax.shard_map(
        fused_step if fused else plain_step,
        mesh=mesh,
        in_specs=(
            P("dp", None),
            P("dp"),
            P(),
            P(None, None, ("dp", "tensor")),
            P(None, None, ("dp", "tensor")),
            P(None, None, "dp", "tensor"),
            P(None, "tensor", "dp"),
            P(None, "dp", "tensor"),
            P(None, "tensor", "dp"),
            P("dp", None),
        ),
        out_specs=(
            P("dp", None),
            P("dp", None),
            P(None, None, ("dp", "tensor")),
            P(None, None, ("dp", "tensor")),
            P(None, None, "dp", "tensor"),
            P(None, "tensor", "dp"),
            P(None, "dp", "tensor"),
            P(None, "tensor", "dp"),
        ),
        check_vma=False,
    )
```

```python
import jax
import jax.numpy as jnp
from jax import lax
from jax.experimental import pallas as pl
from jax.experimental.pallas import tpu as pltpu
from jax.sharding import PartitionSpec as P

D = 768
HEAD_DIM = 64
FF = 3072
NSRC = 4
EPS = 1e-05
MASKED = -1e30
F32 = jnp.float32
BF16 = jnp.bfloat16
VMEM_LIMIT = 60 * 1024 * 1024


def dot_nn(a, b):
    return lax.dot_general(a, b, (((1,), (0,)), ((), ())), preferred_element_type=F32)


def dot_nt(a, b):
    return lax.dot_general(a, b, (((1,), (1,)), ((), ())), preferred_element_type=F32)


def norm_parts(v):
    center = jnp.mean(v, -1, keepdims=True)
    centered = v - center
    r = lax.rsqrt(jnp.mean(centered * centered, -1, keepdims=True) + EPS)
    return centered * r, r


def head_mask(shape, h):
    lane = lax.broadcasted_iota(jnp.int32, shape, 1)
    return (lane >= h * HEAD_DIM) & (lane < (h + 1) * HEAD_DIM)


def blocks(total, size):
    return [slice(i * size, (i + 1) * size) for i in range(total // size)]


def attention_forward(
    len_ref, x_ref, g_ref, rows_ref, bqv_ref,
    q_ref, v_ref, kt_ref, p_ref, o_ref, a1t_ref, h1_ref, a2_ref, a2t_ref,
    a1_ref, k_ref, vt_ref, ot_ref, attn_ref,
):
    t = pl.program_id(0)
    n = x_ref.shape[0]
    width = g_ref.shape[-1]
    heads = width // HEAD_DIM
    step = 256
    length = len_ref[0]

    @pl.when(t == 0)
    def _():
        @pl.loop(0, n // step)
        def _(b):
            rows = pl.ds(pl.multiple_of(b * step, step), step)
            xhat, _ = norm_parts(x_ref[rows, :].astype(F32))
            a1 = xhat * rows_ref[0:1, :] + rows_ref[2:3, :]
            a1_ref[rows, :] = a1.astype(BF16)
            a1t_ref[:, rows] = a1.astype(BF16).T
            attn_ref[rows, :] = x_ref[rows, :].astype(F32) + rows_ref[5:6, :]

    @pl.loop(0, n // step)
    def _(b):
        rows = pl.ds(pl.multiple_of(b * step, step), step)
        a1 = a1_ref[rows, :]
        q = (dot_nn(a1, g_ref[0, 0]) + bqv_ref[0, 0:1, :]).astype(BF16)
        q_ref[0, rows, :] = q * jnp.asarray(HEAD_DIM ** -0.5, BF16)
        k = dot_nn(a1, g_ref[0, 1]).astype(BF16)
        k_ref[rows, :] = k
        kt_ref[0, :, rows] = k.T
        v = (dot_nn(a1, g_ref[0, 2]) + bqv_ref[0, 1:2, :]).astype(BF16)
        v_ref[0, rows, :] = v
        vt_ref[:, rows] = v.T

    for h in range(heads):
        k = k_ref[...]
        k = jnp.where(head_mask(k.shape, h), k, jnp.zeros_like(k))
        for b in range(n // step):
            first, last = b * step, (b + 1) * step
            q = q_ref[0, first:last, :]
            key = lax.broadcasted_iota(jnp.int32, (last, step), 0)
            query = lax.broadcasted_iota(jnp.int32, (step, step), 1) + first
            s = dot_nt(k[:last], q)
            near = jnp.where(
                (key[first:] <= query) & (key[first:] < length), s[first:], MASKED
            )
            if b:
                far = jnp.where(key[:first] < length, s[:first], MASKED)
                top = jnp.maximum(
                    jnp.max(far, 0, keepdims=True), jnp.max(near, 0, keepdims=True)
                )
                e_far = jnp.exp(far - top)
                e_near = jnp.exp(near - top)
                total = jnp.sum(e_far, 0, keepdims=True) + jnp.sum(e_near, 0, keepdims=True)
                scale = 1.0 / total
                p_ref[0, h, :first, first:last] = (e_far * scale).astype(BF16)
            else:
                top = jnp.max(near, 0, keepdims=True)
                e_near = jnp.exp(near - top)
                scale = 1.0 / jnp.sum(e_near, 0, keepdims=True)
            p_ref[0, h, first:last, first:last] = (e_near * scale).astype(BF16)
            ot_ref[h * HEAD_DIM : (h + 1) * HEAD_DIM, first:last] = dot_nn(
                vt_ref[h * HEAD_DIM : (h + 1) * HEAD_DIM, :last],
                p_ref[0, h, :last, first:last],
            ).astype(BF16)

    @pl.loop(0, n // step)
    def _(b):
        rows = pl.ds(pl.multiple_of(b * step, step), step)
        o = ot_ref[:, rows].T
        o_ref[0, rows, :] = o
        attn_ref[rows, :] += dot_nt(o, g_ref[0, 3])

    @pl.when(t == pl.num_programs(0) - 1)
    def _():
        @pl.loop(0, n // step)
        def _(b):
            rows = pl.ds(pl.multiple_of(b * step, step), step)
            h1 = attn_ref[rows, :]
            h1_ref[rows, :] = h1
            xhat, _ = norm_parts(h1)
            a2 = (xhat * rows_ref[1:2, :] + rows_ref[6:7, :]).astype(BF16)
            a2_ref[rows, :] = a2
            a2t_ref[:, rows] = a2.T


SQRT_2_PI = 0.7978845608028654


def feed_forward_both(
    len_ref, c_ref, a2_ref, a2t_ref, h1_ref, w1_ref, w2_ref, rows_ref,
    out_ref, d1_ref, d2_ref, dh1_ref, gb_ref, gbt_ref, sums_ref,
    gf_ref, gft_ref, feed_ref, da2_ref, h_ref, df_ref,
):
    t = pl.program_id(0)
    n = c_ref.shape[0]
    step = 256
    length = len_ref[0]

    @pl.when(t == 0)
    def _():
        sums_ref[...] = jnp.zeros_like(sums_ref)

        @pl.loop(0, n // step)
        def _(b):
            rows = pl.ds(pl.multiple_of(b * step, step), step)
            place = b * step + lax.broadcasted_iota(jnp.int32, (step, 1), 0)
            live = (place < length).astype(F32)
            g = (c_ref[rows, :].astype(F32) * live).astype(BF16)
            gf_ref[rows, :] = g
            gft_ref[:, rows] = g.T
            sums_ref[7:8, :] += jnp.sum(g.astype(F32), 0, keepdims=True)

    bias = rows_ref[pl.ds(8 + t, 1), :]

    @pl.loop(0, n // step)
    def _(b):
        rows = pl.ds(pl.multiple_of(b * step, step), step)
        f = dot_nn(a2_ref[rows, :], w1_ref[0]) + bias
        dh = dot_nn(gf_ref[rows, :], w2_ref[0])
        f2 = f * f
        th = jnp.tanh(f * (SQRT_2_PI + (SQRT_2_PI * 0.044715) * f2))
        half = 0.5 + 0.5 * th
        h = (f * half).astype(BF16)
        slope = half + f * (0.5 - 0.5 * th * th) * (
            SQRT_2_PI + (3 * SQRT_2_PI * 0.044715) * f2
        )
        df = (dh * slope).astype(BF16)
        h_ref[rows, :] = h
        df_ref[rows, :] = df
        sums_ref[pl.ds(8 + t, 1), :] += jnp.sum(df.astype(F32), 0, keepdims=True)
        feed = dot_nt(h, w2_ref[0])
        da2 = dot_nt(df, w1_ref[0])

        @pl.when(t == 0)
        def _():
            feed_ref[rows, :] = feed
            da2_ref[rows, :] = da2

        @pl.when(t > 0)
        def _():
            feed_ref[rows, :] += feed
            da2_ref[rows, :] += da2

    @pl.loop(0, D // step)
    def _(b):
        rows = pl.ds(pl.multiple_of(b * step, step), step)
        d1_ref[0, rows, :] = dot_nn(a2t_ref[rows, :], df_ref[...]).astype(BF16)
        d2_ref[0, rows, :] = dot_nn(gft_ref[rows, :], h_ref[...]).astype(BF16)

    @pl.when(t == pl.num_programs(0) - 1)
    def _():
        @pl.loop(0, n // step)
        def _(b):
            rows = pl.ds(pl.multiple_of(b * step, step), step)
            place = b * step + lax.broadcasted_iota(jnp.int32, (step, 1), 0)
            live = (place < length).astype(F32)
            h1 = h1_ref[rows, :]
            out_ref[rows, :] = (live * (h1 + (feed_ref[rows, :] + rows_ref[7:8, :]))).astype(BF16)
            xhat, r = norm_parts(h1)
            da2 = da2_ref[rows, :]
            sums_ref[1:2, :] += jnp.sum(da2 * xhat, 0, keepdims=True)
            sums_ref[6:7, :] += jnp.sum(da2, 0, keepdims=True)
            dg = da2 * rows_ref[1:2, :]
            dv = r * (
                dg
                - jnp.mean(dg, -1, keepdims=True)
                - xhat * jnp.mean(dg * xhat, -1, keepdims=True)
            )
            dh1 = live * c_ref[rows, :].astype(F32) + dv
            dh1_ref[rows, :] = dh1
            gb = dh1.astype(BF16)
            gb_ref[rows, :] = gb
            gbt_ref[:, rows] = gb.T
            sums_ref[5:6, :] += jnp.sum(gb.astype(F32), 0, keepdims=True)


def attention_backward(
    x_ref, g_ref, rows_ref, dh1_ref, gb_ref, gbt_ref, q_ref, v_ref, kt_ref, p_ref,
    o_ref, a1t_ref,
    d0_ref, xg_ref, sums_ref, bqv_ref,
    do_ref, delta_ref, dqt_ref, dq_ref, dk_ref, dv_ref, da1_ref,
):
    t = pl.program_id(0)
    n = x_ref.shape[0]
    width = g_ref.shape[-1]
    heads = width // HEAD_DIM
    step = 256
    pick = (
        lax.broadcasted_iota(jnp.int32, (16, width), 1) // HEAD_DIM
        == lax.broadcasted_iota(jnp.int32, (16, width), 0)
    ).astype(BF16)

    @pl.loop(0, n // step)
    def _(b):
        rows = pl.ds(pl.multiple_of(b * step, step), step)
        do = dot_nn(gb_ref[rows, :], g_ref[0, 3]).astype(BF16)
        do_ref[rows, :] = do
        prod = do.astype(F32) * o_ref[0, rows, :].astype(F32)
        high = prod.astype(BF16)
        low = (prod - high.astype(F32)).astype(BF16)
        delta_ref[:, rows] = dot_nt(pick, high) + dot_nt(pick, low)

    dqt_ref[...] = jnp.zeros_like(dqt_ref)
    for b in range(n // step):
        first, last = b * step, (b + 1) * step
        do = do_ref[first:, :]
        q = q_ref[0, first:, :]
        v = v_ref[0, first:last, :]
        dk, dv = None, None
        for h in range(heads):
            mine = head_mask((1, width), h)
            zero = jnp.zeros((), BF16)
            p = p_ref[0, h, first:last, first:]
            dp = dot_nt(jnp.where(mine, v, zero), do)
            ds = (p.astype(F32) * (dp - delta_ref[h : h + 1, first:])).astype(BF16)
            part = dot_nn(p, jnp.where(mine, do, zero))
            dv = part if dv is None else dv + part
            part = dot_nn(ds, jnp.where(mine, q, zero))
            dk = part if dk is None else dk + part
            head = slice(h * HEAD_DIM, (h + 1) * HEAD_DIM)
            dqt_ref[head, first:] += dot_nn(kt_ref[0, head, first:last], ds)
        dk_ref[first:last, :] = dk.astype(BF16)
        dv_ref[first:last, :] = dv.astype(BF16)

    @pl.when(t == 0)
    def _():
        da1_ref[...] = jnp.zeros_like(da1_ref)

    bqv_ref[...] = jnp.zeros_like(bqv_ref)

    @pl.loop(0, n // step)
    def _(b):
        rows = pl.ds(pl.multiple_of(b * step, step), step)
        dq = (dqt_ref[:, rows] * HEAD_DIM ** -0.5).astype(BF16).T
        dk = dk_ref[rows, :]
        dv = dv_ref[rows, :]
        dq_ref[rows, :] = dq
        bqv_ref[0, 0:1, :] += jnp.sum(dq.astype(F32), 0, keepdims=True)
        bqv_ref[0, 1:2, :] += jnp.sum(dv.astype(F32), 0, keepdims=True)
        da1_ref[rows, :] += (
            dot_nt(dq, g_ref[0, 0]) + dot_nt(dk, g_ref[0, 1]) + dot_nt(dv, g_ref[0, 2])
        )

    @pl.loop(0, D // step)
    def _(b):
        rows = pl.ds(pl.multiple_of(b * step, step), step)
        a1t = a1t_ref[rows, :]
        d0_ref[0, 0, rows, :] = dot_nn(a1t, dq_ref[...]).astype(BF16)
        d0_ref[0, 1, rows, :] = dot_nn(a1t, dk_ref[...]).astype(BF16)
        d0_ref[0, 2, rows, :] = dot_nn(a1t, dv_ref[...]).astype(BF16)
        d0_ref[0, 3, rows, :] = dot_nn(gbt_ref[rows, :], o_ref[0]).astype(BF16)

    @pl.when(t == pl.num_programs(0) - 1)
    def _():
        sums_ref[...] = jnp.zeros_like(sums_ref)

        @pl.loop(0, n // step)
        def _(b):
            rows = pl.ds(pl.multiple_of(b * step, step), step)
            xhat, r = norm_parts(x_ref[rows, :].astype(F32))
            da1 = da1_ref[rows, :]
            sums_ref[0:1, :] += jnp.sum(da1 * xhat, 0, keepdims=True)
            sums_ref[1:2, :] += jnp.sum(da1, 0, keepdims=True)
            dg = da1 * rows_ref[0:1, :]
            dv = r * (
                dg
                - jnp.mean(dg, -1, keepdims=True)
                - xhat * jnp.mean(dg * xhat, -1, keepdims=True)
            )
            xg_ref[rows, :] = (dh1_ref[rows, :] + dv).astype(BF16)


def whole(*shape):
    return pl.BlockSpec(shape, lambda t: (0,) * len(shape))


def group(*shape):
    return pl.BlockSpec((1,) + shape, lambda t: (t,) + (0,) * len(shape))


def shaped(dtype, *shape):
    return jax.ShapeDtypeStruct(shape, dtype)


SMEM_WHOLE = pl.BlockSpec(memory_space=pltpu.SMEM)


def run_attention_forward(length, x, g0, rows, bqv):
    n = x.shape[0]
    groups, _, _, width = g0.shape
    heads = width // HEAD_DIM
    return pl.pallas_call(
        attention_forward,
        grid=(groups,),
        in_specs=[SMEM_WHOLE, whole(n, D), group(4, D, width), whole(16, D), group(2, width)],
        out_specs=[
            group(n, width), group(n, width), group(width, n), group(heads, n, n),
            group(n, width), whole(D, n), whole(n, D), whole(n, D), whole(D, n),
        ],
        out_shape=[
            shaped(BF16, groups, n, width), shaped(BF16, groups, n, width),
            shaped(BF16, groups, width, n), shaped(BF16, groups, heads, n, n),
            shaped(BF16, groups, n, width), shaped(BF16, D, n), shaped(F32, n, D),
            shaped(BF16, n, D), shaped(BF16, D, n),
        ],
        scratch_shapes=[
            pltpu.VMEM((n, D), BF16), pltpu.VMEM((n, width), BF16),
            pltpu.VMEM((width, n), BF16), pltpu.VMEM((width, n), BF16),
            pltpu.VMEM((n, D), F32),
        ],
        compiler_params=pltpu.CompilerParams(vmem_limit_bytes=VMEM_LIMIT),
        name="attention_forward",
    )(length, x, g0, rows, bqv)


def run_feed_forward(length, cot, a2, a2t, h1, g1, g2, rows):
    n = cot.shape[0]
    groups, _, width = g1.shape
    return pl.pallas_call(
        feed_forward_both,
        grid=(groups,),
        in_specs=[
            SMEM_WHOLE, whole(n, D), whole(n, D), whole(D, n), whole(n, D),
            group(D, width), group(D, width), whole(16, D),
        ],
        out_specs=[
            whole(n, D), group(D, width), group(D, width), whole(n, D), whole(n, D),
            whole(D, n), whole(16, D),
        ],
        out_shape=[
            shaped(BF16, n, D), shaped(BF16, groups, D, width), shaped(BF16, groups, D, width),
            shaped(F32, n, D), shaped(BF16, n, D), shaped(BF16, D, n), shaped(F32, 16, D),
        ],
        scratch_shapes=[
            pltpu.VMEM((n, D), BF16), pltpu.VMEM((D, n), BF16), pltpu.VMEM((n, D), F32),
            pltpu.VMEM((n, D), F32), pltpu.VMEM((n, width), BF16), pltpu.VMEM((n, width), BF16),
        ],
        compiler_params=pltpu.CompilerParams(vmem_limit_bytes=VMEM_LIMIT),
        name="feed_forward_both",
    )(length, cot, a2, a2t, h1, g1, g2, rows)


def run_attention_backward(x, g0, rows, dh1, gb, gbt, q, v, kt, p, o, a1t):
    n = x.shape[0]
    groups, _, _, width = g0.shape
    heads = width // HEAD_DIM
    return pl.pallas_call(
        attention_backward,
        grid=(groups,),
        in_specs=[
            whole(n, D), group(4, D, width), whole(16, D), whole(n, D), whole(n, D),
            whole(D, n), group(n, width), group(n, width), group(width, n),
            group(heads, n, n), group(n, width), whole(D, n),
        ],
        out_specs=[group(4, D, width), whole(n, D), whole(8, D), group(8, width)],
        out_shape=[
            shaped(BF16, groups, 4, D, width), shaped(BF16, n, D), shaped(F32, 8, D),
            shaped(F32, groups, 8, width),
        ],
        scratch_shapes=[
            pltpu.VMEM((n, width), BF16), pltpu.VMEM((16, n), F32), pltpu.VMEM((width, n), F32),
            pltpu.VMEM((n, width), BF16), pltpu.VMEM((n, width), BF16),
            pltpu.VMEM((n, width), BF16), pltpu.VMEM((n, D), F32),
        ],
        compiler_params=pltpu.CompilerParams(vmem_limit_bytes=VMEM_LIMIT),
        name="attention_backward",
    )(x, g0, rows, dh1, gb, gbt, q, v, kt, p, o, a1t)


Z_DEV, Y_DEV, X_DEV, C_DEV = 4, 2, 2, 2


class Place:
    def __init__(self):
        dp, self.t = lax.axis_index("dp"), lax.axis_index("tensor")
        self.dp = dp
        self.z, self.y = dp // 2, dp % 2
        self.x, self.c = self.t // 2, self.t % 2
        self.other_y = 1 - self.y
        self.zs = [
            self.z,
            self.z + 1 - 2 * (self.z % 2),
            self.z + 2 - 4 * (self.z // 2),
            3 - self.z,
        ]
        self.ts = [
            self.t,
            self.t + 1 - 2 * (self.t % 2),
            self.t + 2 - 4 * (self.t // 2),
            3 - self.t,
        ]
        self.to_z = [dict(dp=z * 2 + self.y) for z in self.zs]
        self.to_y = dict(dp=self.z * 2 + self.other_y)
        self.to_x = dict(tensor=self.ts[2])
        self.same_t = self.to_z[1:] + [dict(dp=z * 2 + self.other_y) for z in self.zs]
        self.same_dp = [dict(tensor=t) for t in self.ts[1:]]
        self.to_core = dict(tensor=self.ts[1])

    def group(self, k):
        return lax.select(
            k == 0, self.ts[0],
            lax.select(k == 1, self.ts[1], lax.select(k == 2, self.ts[2], self.ts[3])),
        )

    def greet(self, others=None):
        barrier = pltpu.get_barrier_semaphore()
        others = others or self.to_z[1:] + [self.to_y, self.to_x, self.to_core]
        for device in others:
            pl.semaphore_signal(
                barrier, inc=1, device_id=device, device_id_type=pl.DeviceIdType.MESH
            )
        pl.semaphore_wait(barrier, len(others))


class Pieces:
    def __init__(self, whole, pieces):
        self.whole, self.pieces = whole, pieces

    def start(self):
        for piece in self.pieces:
            piece.start()

    def wait_recv(self):
        self.whole.wait_recv()

    def wait_send(self):
        self.whole.wait_send()


class Links:
    def __init__(self, send_sem, recv_sem):
        self.send_sem, self.recv_sem = send_sem, recv_sem
        self.copies = []

    def add(self, device, src, dst, parts=1, axis=0):
        number = len(self.copies)

        def make(src, dst):
            return pltpu.make_async_remote_copy(
                src_ref=src,
                dst_ref=dst,
                send_sem=self.send_sem.at[number],
                recv_sem=self.recv_sem.at[number],
                device_id=device,
                device_id_type=pl.DeviceIdType.MESH,
            )

        size = src.shape[axis] // parts
        cuts = [(slice(None),) * axis + (pl.ds(i * size, size),) for i in range(parts)]
        copy = Pieces(make(src, dst), [make(src.at[cut], dst.at[cut]) for cut in cuts])
        self.copies.append(copy)
        return copy

    def sent(self, *apart):
        for copy in self.copies:
            if all(copy is not other for other in apart):
                copy.wait_send()


def flat(copies):
    for item in copies:
        if isinstance(item, list):
            yield from flat(item)
        else:
            yield item


def start(*copies):
    for copy in flat(copies):
        copy.start()


def recv(*copies):
    for copy in flat(copies):
        copy.wait_recv()


class Gather:
    def __init__(self, links, place, own, full, order, single=True, last=True):
        every = slice(None)
        y, other = place.y, place.other_y

        def same(device, k, yy, to):
            return links.add(device, full(k, every, yy), full(to, every, yy), Z_DEV)

        def along_z(k, yy, block):
            here, passed = full(k, place.z, yy), full(k, place.zs[2], yy)
            return [
                links.add(place.to_z[1], block, here, 2),
                links.add(place.to_z[2], block, here, 2),
                links.add(place.to_z[1], passed, passed, 2),
            ]

        self.z = along_z(0, y, own)
        if order == X_Z_Y:
            self.first = [links.add(place.to_x, own, full(2, place.z, y), 2)]
            self.far = along_z(2, y, full(2, place.z, y))
            blocks = [(0, y), (2, y), (0, other), (2, other)]
        else:
            blocks = [(0, y), (0, other), (2, y), (2, other)]
        if order == Y_Z_X:
            self.first = [links.add(place.to_y, own, full(0, place.z, y), 2)]
            self.far = along_z(0, other, full(0, place.z, other))
        if order == Z_Y_X and single:
            self.first = [same(place.to_y, 0, y, 0)]
        if order == Z_Y_X and not single:
            self.first = [links.add(place.to_y, own, full(0, place.z, y), 2)]
            for k in range(1, 4):
                block = full(0, place.zs[k], y)
                self.first.append(links.add(place.to_y, block, block, 2))
        self.second = [
            same(place.to_y, k, yy, k) if order == X_Z_Y else same(place.to_x, k, yy, 2)
            for k, yy in blocks[: 2 if last else 1]
        ]
        if not last:
            blocks = [block for block in blocks if block[0] == 0]
        self.core = [same(place.to_core, k, yy, k + 1) for k, yy in blocks]


Z_Y_X, Y_Z_X, X_Z_Y = range(3)


def fused_forward(
    tie_ref, len_ref, tokens_ref, gains_ref, bias_ref, in_ref, out_ref, expand_ref,
    project_ref,
    gq_ref, gw_ref, flat1_ref, flat2_ref, rows_ref,
    q_ref, v_ref, kt_ref, p_ref, scale_ref, o_ref, a1t_out, h1_out, a2_out, a2t_out,
    own0_ref, ownw_ref, own1_ref, own2_ref, square_ref, vec_ref,
    all0_ref, allw_ref, w1_ref, w2_ref, vecs_ref, bqv_ref, x_ref, a1_ref, k_ref, qa_ref, vt_ref, ot_ref, a1t_ref, h1_ref, a2_ref, a2t_ref,
    send_sem, recv_sem, local_sem, flush_sem, row_sem,
):
    t = pl.program_id(0)
    n, _ = x_ref.shape
    width = allw_ref.shape[-1]
    heads = width // HEAD_DIM
    step = 256
    place = Place()
    length = len_ref[place.t]
    links = Links(send_sem, recv_sem)
    z, y, x, c = place.z, place.y, place.x, place.c
    mine_there = vecs_ref.at[z, y, x, c]
    column = vecs_ref.at[:, :, x, c]
    vec_one = [links.add(device, vec_ref, mine_there) for device in place.same_t]
    vec_two = [links.add(device, column, column) for device in place.same_dp]
    seg0 = Gather(
        links, place, own0_ref, lambda k, z, y: all0_ref.at[k, z, y], Z_Y_X, single=False
    )
    segw = Gather(links, place, ownw_ref, lambda k, z, y: allw_ref.at[k, z, y], Z_Y_X)
    seg1 = Gather(
        links, place, own1_ref, lambda k, z, y: w1_ref.at[k, z, y], Y_Z_X, last=False
    )
    seg2 = Gather(
        links, place, own2_ref, lambda k, z, y: w2_ref.at[k, z, y], X_Z_Y, last=False
    )
    flush = [
        [
            pltpu.make_async_copy(ref.at[k], flat.at[k], flush_sem.at[i, k])
            for k in range(3)
        ]
        for i, (ref, flat) in enumerate([(w1_ref, flat1_ref), (w2_ref, flat2_ref)])
    ]
    put_a1t = pltpu.make_async_copy(a1t_ref, a1t_out, local_sem.at[0])
    put_a2t = pltpu.make_async_copy(a2t_ref, a2t_out, local_sem.at[1])
    puts = []
    for i in range(n // step):
        rows = pl.ds(i * step, step)
        puts.append([
            pltpu.make_async_copy(h1_ref.at[rows], h1_out.at[rows], row_sem.at[0, i]),
            pltpu.make_async_copy(a2_ref.at[rows], a2_out.at[rows], row_sem.at[1, i]),
        ])
    fetch = pltpu.make_async_copy(tokens_ref.at[place.t], x_ref, local_sem.at[2])

    def relay_z(copies):
        recv(copies[1])
        start(copies[2])

    def pass_own(seg):
        recv(seg.z[0], seg.z[2])
        if seg is segw:
            start(seg.first)
        start(seg.second[0], seg.core[0])

    def pass_second(seg):
        recv(seg.second)
        if seg is seg2:
            start(seg.core[1])

    def pass_first(seg):
        recv(seg.first)
        if seg is segw:
            start(seg.second[1], seg.core[1])
        else:
            start(seg.far[1], seg.far[0])

    def pass_far(seg):
        recv(seg.far[0], seg.far[2])
        start(seg.core[1:] if seg is seg1 else [])

    def pass_core(seg, i):
        recv(seg.second[i])
        start(seg.core[2 + i])

    plan = [
        (0, 0, lambda: (pass_own(segw), pass_first(seg1), relay_z(seg2.z), pass_first(seg2))),
        (0, 2, lambda: (pass_first(segw), relay_z(seg1.z), pass_core(seg0, 0))),
        (1, 0, lambda: recv(seg0.core[:2])),
        (1, 1, lambda: relay_z(seg1.far)),
        (1, 2, lambda: (
            pass_core(seg0, 1), recv(segw.core[:2]), pass_core(segw, 0), pass_own(seg2),
        )),
        (2, 1, lambda: relay_z(seg2.far)),
        (2, 2, lambda: (pass_core(segw, 1), pass_own(seg1))),
        (3, 0, lambda: (recv(seg0.core[2:]), pass_far(seg1), flush[0][0].start())),
        (3, 1, lambda: (pass_second(seg2), flush[1][0].start())),
        (3, 2, lambda: (pass_far(seg2), flush[1][2].start(), recv(segw.core[2:]))),
    ]

    def serve(point):
        for step, where, act in plan:
            if where == point:
                pl.when(t == step)(lambda act=act: (act(), None)[1])

    @pl.when(t == 0)
    def _():
        s0, s1, s2, s3 = tie_ref[0], tie_ref[1], tie_ref[2], tie_ref[3]
        fetch.start()
        square_ref[...] = jnp.zeros_like(square_ref)
        gain = gains_ref.shape[-1]
        square_ref[0:1, :gain] = gains_ref[s0].astype(F32)[0:1]
        square_ref[1:2, :gain] = gains_ref[s2].astype(F32)[1:2]
        kinds = [s0, s0, s0, s1, s2, s3, s2, s2, s2, s2]
        for i, source in enumerate(kinds):
            wide = bias_ref[i].astype(F32)
            here = lax.broadcasted_iota(jnp.int32, wide.shape, 0) == source
            square_ref[2 + i : 3 + i, :gain] = jnp.sum(
                jnp.where(here, wide, 0.0), 0, keepdims=True
            )
        vec_ref[...] = square_ref[...].T[:gain]
        for j in range(3):
            own0_ref[:, j * width : (j + 1) * width] = in_ref[s0, j]
        place.greet(place.same_t + place.same_dp)
        start(vec_one, seg0.z[1], seg0.z[0], seg0.first[0])
        vecs_ref[z, y, x, c] = vec_ref[...]
        ones = lax.broadcasted_iota(jnp.int32, (vt_ref.shape[1] - HEAD_DIM, n), 0) == 0
        for h in range(heads):
            vt_ref[h, HEAD_DIM:, :] = ones.astype(BF16)
        all0_ref[0, z, y] = own0_ref[...]
        ownw_ref[...] = out_ref[s1].T
        allw_ref[0, z, y] = ownw_ref[...]
        own1_ref[...] = expand_ref[s2]
        own2_ref[...] = project_ref[s3]
        w1_ref[0, z, y] = own1_ref[...]
        w2_ref[0, z, y] = own2_ref[...]
        recv(vec_one)
        start(vec_two)
        relay_z(seg0.z)
        start(seg0.first[2])
        recv(seg0.z[0])
        start(seg0.first[1], segw.z[1], segw.z[0], seg2.z[1])
        recv(vec_two)
        start(seg2.first)
        vecs = vecs_ref[...].reshape(D, vecs_ref.shape[-1]).T[:16]
        rows_ref[...] = vecs
        recv(seg0.z[2])
        start(seg0.first[3], seg1.first, seg0.second[0], seg0.core[0])
        for k in range(4):
            part = slice(k * width, (k + 1) * width)
            bqv_ref[k, 0:1, :width] = vecs[3:4, part]
            bqv_ref[k, 0:1, width : 2 * width] = jnp.zeros((1, width), F32)
            bqv_ref[k, 0:1, 2 * width :] = vecs[4:5, part]
        fetch.wait()

        @pl.loop(0, n // step)
        def _(b):
            rows = pl.ds(pl.multiple_of(b * step, step), step)
            wide = x_ref[rows, :].astype(F32)
            xhat, _ = norm_parts(wide)
            a1 = (xhat * rows_ref[0:1, :] + rows_ref[2:3, :]).astype(BF16)
            a1_ref[rows, :] = a1
            a1t_ref[:, rows] = a1.T
            h1_ref[rows, :] = wide + rows_ref[5:6, :]

        put_a1t.start()
        relay_z(segw.z)
        start(seg2.z[0], seg1.z[1], seg1.z[0])
        recv(seg0.first)
        start(seg0.second[1], seg0.core[1])

    serve(0)
    gq = all0_ref[t].reshape(D, 3 * width)
    gq_ref[0] = gq
    mine = place.group(t)
    qkv = dot_nn(a1_ref[...], gq) + bqv_ref[mine, 0:1, :]
    q = qkv[:, :width].astype(BF16) * jnp.asarray(HEAD_DIM ** -0.5, BF16)
    k = qkv[:, width : 2 * width].astype(BF16)
    v = qkv[:, 2 * width :].astype(BF16)
    q_ref[0] = q
    kt_ref[0] = k.T
    v_ref[0] = v
    vt = v.T
    for h in range(heads):
        vt_ref[h, :HEAD_DIM, :] = vt[h * HEAD_DIM : (h + 1) * HEAD_DIM]
    spare = k_ref.shape[1] - width
    dead = lax.broadcasted_iota(jnp.int32, (n, spare), 0) >= length
    first_column = lax.broadcasted_iota(jnp.int32, (n, spare), 1) == 0
    k_ref[:, :width] = k
    k_ref[:, width:] = jnp.where(first_column & dead, MASKED, 0.0).astype(BF16)
    qa_ref[:, :width] = q
    qa_ref[:, width:] = jnp.where(first_column, 1.0, 0.0).astype(BF16)

    serve(1)
    def scores(h, b):
        first, last = b * step, (b + 1) * step
        q = qa_ref[first:last, :]
        lane = lax.broadcasted_iota(jnp.int32, (1, q.shape[1]), 1)
        keep = head_mask((1, q.shape[1]), h) | (lane >= width)
        return dot_nt(k_ref[:last, :], jnp.where(keep, q, jnp.zeros((), BF16)))

    def attend(h, b, s):
        first, last = b * step, (b + 1) * step
        key = lax.broadcasted_iota(jnp.int32, (step, step), 0)
        query = lax.broadcasted_iota(jnp.int32, (step, step), 1)
        near = jnp.where(key <= query, s[first:], MASKED)
        top = jnp.max(near, 0, keepdims=True)
        if b:
            far = s[:first]
            top = jnp.maximum(top, jnp.max(far, 0, keepdims=True))
        e_near = jnp.exp((near - top).astype(BF16))
        p_ref[0, h, b, first:last, :] = e_near
        o = dot_nn(vt_ref[h, :, first:last], e_near)
        if b:
            e_far = jnp.exp((far - top).astype(BF16))
            p_ref[0, h, b, :first, :] = e_far
            o += dot_nn(vt_ref[h, :, :first], e_far)
        scale = 1.0 / o[HEAD_DIM : HEAD_DIM + 1]
        scale_ref[0, h : h + 1, first:last] = scale
        ot_ref[h * HEAD_DIM : (h + 1) * HEAD_DIM, first:last] = (
            o[:HEAD_DIM] * scale
        ).astype(BF16)

    scale_ref[0, heads:, :] = jnp.zeros((scale_ref.shape[1] - heads, n), F32)
    ready = [scores(h, 0) for h in range(heads)]
    for b in range(n // step):
        ahead = [scores(h, b + 1) for h in range(heads)] if b + 1 < n // step else None
        for h in range(heads):
            attend(h, b, ready[h])
        ready = ahead
    serve(2)

    gw_ref[0] = allw_ref[t].reshape(gw_ref.shape[1:])
    o = ot_ref[...].T
    o_ref[0] = o
    h1_ref[...] += dot_nt(o, gw_ref[0])

    @pl.when(t == 3)
    def _():
        for i, rows in enumerate(blocks(n, step)):
            xhat, _ = norm_parts(h1_ref[rows, :])
            a2 = (xhat * rows_ref[1:2, :] + rows_ref[6:7, :]).astype(BF16)
            a2_ref[rows, :] = a2
            a2t_ref[:, rows] = a2.T
            for put in puts[i]:
                put.start()
        put_a2t.start()
        recv(seg2.core)
        flush[1][1].start()
        recv(seg1.core)
        flush[0][1].start()
        pass_second(seg1)
        flush[0][2].start()
        links.sent()
        for copies in flush + puts + [[put_a1t, put_a2t]]:
            for copy in copies:
                copy.wait()


N_GATHER = 10 + 13 + 10 + 10 + 10
VMEM_WHOLE = pl.BlockSpec(memory_space=pltpu.VMEM)
ANY_WHOLE = pl.BlockSpec(memory_space=pl.ANY)


def run_fused_forward(tie, lengths, tokens, gains, biases, w_in, w_out, w_expand, w_project):
    groups, n, _ = tokens.shape
    depth, width = w_in.shape[-2:]
    heads = width // HEAD_DIM
    hidden = w_expand.shape[-1]
    w_project = w_project.transpose(0, 2, 1)
    biases = biases.transpose(1, 0, 2)
    own = gains.shape[-1]
    return pl.pallas_call(
        fused_forward,
        grid=(groups,),
        in_specs=[SMEM_WHOLE, SMEM_WHOLE, ANY_WHOLE] + [VMEM_WHOLE] * 6,
        out_specs=[
            group(D, 3 * width), group(D, width), ANY_WHOLE, ANY_WHOLE, VMEM_WHOLE,
            group(n, width), group(n, width), group(width, n), group(heads, n // 256, n, 256),
            group(8, n), group(n, width), ANY_WHOLE, ANY_WHOLE, ANY_WHOLE, ANY_WHOLE,
        ],
        out_shape=[
            shaped(BF16, groups, D, 3 * width), shaped(BF16, groups, D, width),
            shaped(BF16, groups, Z_DEV, Y_DEV, depth, hidden),
            shaped(BF16, groups, Z_DEV, Y_DEV, depth, hidden),
            shaped(F32, 16, D),
            shaped(BF16, groups, n, width), shaped(BF16, groups, n, width),
            shaped(BF16, groups, width, n), shaped(BF16, groups, heads, n // 256, n, 256),
            shaped(F32, groups, 8, n), shaped(BF16, groups, n, width), shaped(BF16, D, n), shaped(F32, n, D),
            shaped(BF16, n, D), shaped(BF16, D, n),
        ],
        scratch_shapes=[
            pltpu.VMEM((depth, 3 * width), BF16), pltpu.VMEM((depth, width), BF16),
            pltpu.VMEM((depth, hidden), BF16), pltpu.VMEM((depth, hidden), BF16),
            pltpu.VMEM((128, 128), F32), pltpu.VMEM((own, 128), F32),
            pltpu.VMEM((groups, Z_DEV, Y_DEV, depth, 3 * width), BF16),
            pltpu.VMEM((groups, Z_DEV, Y_DEV, depth, width), BF16),
            pltpu.VMEM((groups, Z_DEV, Y_DEV, depth, hidden), BF16),
            pltpu.VMEM((groups, Z_DEV, Y_DEV, depth, hidden), BF16),
            pltpu.VMEM((Z_DEV, Y_DEV, X_DEV, C_DEV, own, 128), F32),
            pltpu.VMEM((groups, 8, 3 * width), F32),
            pltpu.VMEM((n, D), BF16), pltpu.VMEM((n, D), BF16), pltpu.VMEM((n, 256), BF16),
            pltpu.VMEM((n, 256), BF16), pltpu.VMEM((heads, HEAD_DIM + 16, n), BF16),
            pltpu.VMEM((width, n), BF16),
            pltpu.VMEM((D, n), BF16), pltpu.VMEM((n, D), F32), pltpu.VMEM((n, D), BF16),
            pltpu.VMEM((D, n), BF16),
            pltpu.SemaphoreType.DMA((N_GATHER,)), pltpu.SemaphoreType.DMA((N_GATHER,)),
            pltpu.SemaphoreType.DMA((3,)), pltpu.SemaphoreType.DMA((2, 4)),
            pltpu.SemaphoreType.DMA((2, n // 256)),
        ],
        compiler_params=pltpu.CompilerParams(
            vmem_limit_bytes=VMEM_LIMIT, collective_id=0, has_side_effects=True
        ),
        name="fused_forward",
    )(tie, lengths, tokens, gains, biases, w_in, w_out, w_expand, w_project)


class Result:
    def __init__(self, links, place, own_ref, passing_ref, out_ref, step, sem, count):
        self.x, self.core, self.far, self.keep, self.keep_far = [], [], [], [], []
        for i in range(count):
            rows = pl.ds(i * step, step)
            mine, theirs = out_ref.at[place.t, rows], out_ref.at[place.ts[2], rows]
            own, passing = own_ref.at[rows], passing_ref.at[rows]
            self.x.append(links.add(place.to_x, own, passing))
            self.core.append(links.add(place.to_core, own, mine))
            self.far.append(links.add(place.to_core, passing, theirs))
            self.keep.append(pltpu.make_async_copy(own, mine, sem.at[0, i]))
            self.keep_far.append(pltpu.make_async_copy(passing, theirs, sem.at[1, i]))

    def send(self, i):
        start(self.x[i], self.core[i], self.keep[i])

    def pass_on(self, i):
        recv(self.x[i])
        start(self.far[i], self.keep_far[i])

    def finish(self):
        recv(self.core, self.far)
        for copy in self.keep + self.keep_far:
            copy.wait()


def low(value):
    return jnp.asarray(value, BF16)


def pair_order(i):
    return i + 1 - 2 * (i % 2)


def fused_feed_forward(
    len_ref, cot_ref, a2_ref, a2t_in, h1_in, far1_ref, far2_ref, rows_ref,
    result_out, rest_out, fold_ref, work_out, dh1_out, gb_out, gbt_out, sums_ref,
    gf_ref, gft_ref, feed_ref, da2_ref, h_ref, df_ref, weights_ref, missing_ref, third_ref,
    stage_ref, land_ref, near_ref, cross_ref, a2t_ref, h1_ref, out_ref, work_ref,
    passing_ref, send_sem, recv_sem, local_sem, row_sem, result_sem,
):
    t = pl.program_id(0)
    n = gf_ref.shape[0]
    step = 256
    depth = stage_ref.shape[-2]
    place = Place()
    length = len_ref[place.t]
    links = Links(send_sem, recv_sem)
    y, other = place.y, place.other_y
    last = [
        links.add(place.to_x, far1_ref.at[0, :, other], missing_ref.at[0, 0], Z_DEV),
        links.add(place.to_y, far2_ref.at[2, :, y], missing_ref.at[1, 0], Z_DEV),
    ]
    last_core = [
        links.add(place.to_core, missing_ref.at[i, 0], missing_ref.at[i, 1], Z_DEV)
        for i in range(2)
    ]
    third = [
        links.add(place.to_core, far_ref.at[2, :, y], third_ref.at[i], Z_DEV)
        for i, far_ref in enumerate([far1_ref, far2_ref])
    ]
    core = [
        [
            links.add(place.to_core, stage_ref.at[i], land_ref.at[s, i], Z_DEV) for i in range(2)
        ]
        for s in range(2)
    ]
    cross = [
        links.add(place.to_y, near_ref.at[i, :, other], cross_ref.at[i], Z_DEV)
        for i in range(2)
    ]
    out = Result(links, place, out_ref, passing_ref, result_out, step, result_sem, 1)
    fetch = pltpu.make_async_copy(cot_ref.at[place.t], gf_ref, local_sem.at[0])
    gb_ref, gbt_ref, dh1_ref = gf_ref, gft_ref, da2_ref
    late = [
        pltpu.make_async_copy(a2t_in, a2t_ref, local_sem.at[5]),
        pltpu.make_async_copy(h1_in, h1_ref, local_sem.at[6]),
    ]
    puts = []
    for i in range(n // step):
        rows = pl.ds(i * step, step)
        puts.append([
            pltpu.make_async_copy(ref.at[rows], out.at[rows], row_sem.at[j, i])
            for j, (ref, out) in enumerate(
                [(dh1_ref, dh1_out), (gb_ref, gb_out)]
            )
        ])
    put_gbt = pltpu.make_async_copy(gbt_ref, gbt_out, local_sem.at[7])
    put_work = pltpu.make_async_copy(work_ref, work_out, local_sem.at[8])
    put_rest = pltpu.make_async_copy(
        out_ref.at[pl.ds(step, n - step)], rest_out, local_sem.at[9]
    )
    k = pair_order(t)
    mine = place.group(k)

    def load(step, whole, slot):
        for i, far_ref in enumerate([far1_ref, far2_ref]):
            group = far_ref.at[pair_order(step)]
            to = weights_ref.at[slot, i]
            if not whole:
                group, to = group.at[:, y], to.at[:, y]
            yield pltpu.make_async_copy(group, to, local_sem.at[1 + 2 * slot + i])

    def live_rows(b):
        at = b * step + lax.broadcasted_iota(jnp.int32, (step, 1), 0)
        return (at < length).astype(F32)

    @pl.when(t == 0)
    def _():
        fetch.start()
        for copy in load(0, True, 0):
            copy.start()
        for copy in late:
            copy.start()
        place.greet()
        start(last, third)
        sums_ref[...] = jnp.zeros_like(sums_ref)
        feed_ref[...] = jnp.zeros_like(feed_ref)
        da2_ref[...] = jnp.zeros_like(da2_ref)
        fetch.wait()

        @pl.loop(0, n // step)
        def _(b):
            rows = pl.ds(pl.multiple_of(b * step, step), step)
            g = (gf_ref[rows, :].astype(F32) * live_rows(b)).astype(BF16)
            gf_ref[rows, :] = g
            gft_ref[:, rows] = g.T
            sums_ref[7:8, :] += jnp.sum(g.astype(F32), 0, keepdims=True)

    for i in range(4):
        @pl.when(t == i)
        def _():
            if i == 2:
                recv(last_core, third)
            else:
                for copy in load(i, i < 2, i % 2):
                    copy.wait()
            if i in (0, 2):
                for copy in load(i + 1, i + 1 < 2, (i + 1) % 2):
                    copy.start()
            for j in range(2):
                if i == 2:
                    weights_ref[0, j, :, y] = third_ref[j]
                if i >= 2:
                    weights_ref[i % 2, j, :, other] = missing_ref[j, 3 - i]

    bias = rows_ref[pl.ds(8 + mine, 1), :]
    w1 = weights_ref[t % 2, 0].reshape(D, -1)
    w2 = weights_ref[t % 2, 1].reshape(D, -1)

    def bend(f):
        f = f.astype(BF16)
        f2 = f * f
        th = jnp.tanh(f * (low(SQRT_2_PI) + low(SQRT_2_PI * 0.044715) * f2))
        half = low(0.5) + low(0.5) * th
        slope = half + f * (low(0.5) - low(0.5) * th * th) * (
            low(SQRT_2_PI) + low(3 * SQRT_2_PI * 0.044715) * f2
        )
        return f * half, slope

    @pl.when(t < 3)
    def _():
        column = jnp.zeros((1, w1.shape[1]), F32)
        for rows in blocks(n, step):
            f = dot_nn(a2_ref[rows, :], w1) + bias
            dh = dot_nn(gf_ref[rows, :], w2)
            h, slope = bend(f)
            df = (dh * slope.astype(F32)).astype(BF16)
            h_ref[rows, :] = h
            df_ref[rows, :] = df
            column += jnp.sum(df.astype(F32), 0, keepdims=True)
            feed_ref[rows, :] += dot_nt(h, w2)
            da2_ref[rows, :] += dot_nt(df, w1)
        sums_ref[pl.ds(8 + mine, 1), :] = column

    @pl.when(t == 3)
    def _():
        late[1].wait()
        for i, rows in enumerate(blocks(n, step)):
            h, slope = bend(dot_nn(a2_ref[rows, :], w1) + bias)
            h_ref[rows, :] = h
            df_ref[rows, :] = slope
            total = h1_ref[rows, :] + ((feed_ref[rows, :] + dot_nt(h, w2)) + rows_ref[7:8, :])
            out_ref[rows, :] = (live_rows(i) * total).astype(BF16)
            if i == 0:
                out.send(0)
        put_rest.start()
        column = jnp.zeros((1, w1.shape[1]), F32)
        for rows in blocks(n, step):
            dh = dot_nn(gf_ref[rows, :], w2)
            df = (dh * df_ref[rows, :].astype(F32)).astype(BF16)
            df_ref[rows, :] = df
            column += jnp.sum(df.astype(F32), 0, keepdims=True)
            da2_ref[rows, :] += dot_nt(df, w1)
        sums_ref[pl.ds(8 + mine, 1), :] = column

    @pl.when(t == 1)
    def _():
        recv(last)
        start(last_core)

    @pl.when(t == 0)
    def _():
        late[0].wait()

    def weight_grad(left_ref, right_ref):
        value = dot_nn(left_ref[...], right_ref[...])
        return value.reshape(Z_DEV, Y_DEV, depth, value.shape[-1]).astype(BF16)

    grad1 = weight_grad(a2t_ref, df_ref)
    grad2 = weight_grad(gft_ref, h_ref)

    def put(ref):
        ref[0] = grad1
        ref[1] = grad2

    def reduced(ref):
        return lambda i, s, z: (
            ref[i, z].astype(F32) + land_ref[s, i, z].astype(F32)
        ).astype(BF16)

    @pl.when(t == 0)
    def _():
        put(stage_ref)
        start(core[0])

    @pl.when(t == 1)
    def _():
        put(near_ref)
        recv(core[0])

        @pl.loop(0, Z_DEV)
        def _(z):
            for i in range(2):
                near_ref[i, z] = reduced(near_ref)(i, 0, z)

        start(cross)

    @pl.when(t == 2)
    def _():
        for copy in core[0]:
            copy.wait_send()
        put(stage_ref)
        start(core[1])

    @pl.when(t == 3)
    def _():
        put(work_ref)
        for i, rows in enumerate(blocks(n, step)):
            xhat, r = norm_parts(h1_ref[rows, :])
            da2 = da2_ref[rows, :]
            sums_ref[1:2, :] += jnp.sum(da2 * xhat, 0, keepdims=True)
            sums_ref[6:7, :] += jnp.sum(da2, 0, keepdims=True)
            dg = da2 * rows_ref[1:2, :]
            dv = r * (
                dg
                - jnp.mean(dg, -1, keepdims=True)
                - xhat * jnp.mean(dg * xhat, -1, keepdims=True)
            )
            dh1 = gf_ref[rows, :].astype(F32) + dv
            dh1_ref[rows, :] = dh1
            gb = dh1.astype(BF16)
            gb_ref[rows, :] = gb
            gbt_ref[:, rows] = gb.T
            sums_ref[5:6, :] += jnp.sum(gb.astype(F32), 0, keepdims=True)
            for copy in puts[i]:
                copy.start()
        put_gbt.start()
        recv(core[1])

        @pl.loop(0, Z_DEV)
        def _(z):
            for i in range(2):
                work_ref[i, z] = reduced(work_ref)(i, 1, z)

        put_work.start()
        recv(cross)

        @pl.loop(0, Z_DEV)
        def _(z):
            for i in range(2):
                fold_ref[i, z] = (
                    near_ref[i, z, y].astype(F32) + cross_ref[i, z].astype(F32)
                ).astype(BF16)

        out.pass_on(0)
        out.finish()
        links.sent(*core[0])
        for copies in puts + [[put_gbt, put_work, put_rest]]:
            for copy in copies:
                copy.wait()


def run_fused_feed_forward(lengths, cot, a2, a2t, h1, g1, g2, rows):
    n = cot.shape[1]
    groups, _, _, depth, hidden = g1.shape
    both = (2, Z_DEV, Y_DEV, depth, hidden)
    fold = (2, Z_DEV, depth, hidden)
    return pl.pallas_call(
        fused_feed_forward,
        grid=(groups,),
        in_specs=[SMEM_WHOLE, ANY_WHOLE, VMEM_WHOLE] + [ANY_WHOLE] * 4 + [VMEM_WHOLE],
        out_specs=[ANY_WHOLE] * 2 + [VMEM_WHOLE] + [ANY_WHOLE] * 4 + [VMEM_WHOLE],
        out_shape=[
            shaped(BF16, groups, n // 4, D), shaped(BF16, n - n // 4, D), shaped(BF16, *fold),
            shaped(BF16, *both), shaped(F32, n, D),
            shaped(BF16, n, D), shaped(BF16, D, n), shaped(F32, 16, D),
        ],
        scratch_shapes=[
            pltpu.VMEM((n, D), BF16), pltpu.VMEM((D, n), BF16), pltpu.VMEM((n, D), F32),
            pltpu.VMEM((n, D), F32), pltpu.VMEM((n, hidden), BF16), pltpu.VMEM((n, hidden), BF16),
            pltpu.VMEM((2,) + both, BF16),
            pltpu.VMEM((2,) + fold, BF16), pltpu.VMEM(fold, BF16), pltpu.VMEM(both, BF16),
            pltpu.VMEM((2,) + both, BF16),
            pltpu.VMEM(both, BF16), pltpu.VMEM(fold, BF16),
            pltpu.VMEM((D, n), BF16), pltpu.VMEM((n, D), F32), pltpu.VMEM((n, D), BF16),
            pltpu.VMEM(both, BF16), pltpu.VMEM((n // 4, D), BF16),
            pltpu.SemaphoreType.DMA((15,)), pltpu.SemaphoreType.DMA((15,)),
            pltpu.SemaphoreType.DMA((10,)), pltpu.SemaphoreType.DMA((2, n // 256)),
            pltpu.SemaphoreType.DMA((2, 1)),
        ],
        compiler_params=pltpu.CompilerParams(
            vmem_limit_bytes=VMEM_LIMIT, collective_id=1, has_side_effects=True
        ),
        name="fused_feed_forward",
    )(lengths, cot, a2, a2t, h1, g1, g2, rows)
class Reduce:
    def __init__(
        self, links, place, work, acc, cross_ref, far_ref, mid_ref, last_ref, side_ref,
        slots=(0, 1),
    ):
        self.place, self.work, self.acc = place, work, acc
        self.cross_ref, self.far_ref, self.mid_ref = cross_ref, far_ref, mid_ref
        self.last_ref, self.side_ref = last_ref, side_ref
        zs = place.zs
        self.y = {
            s: [
                links.add(
                    place.to_y, work(s, zs[j], place.other_y), cross_ref.at[s, zs[j]], 2
                )
                for j in (1, 3, 2, 0)
            ]
            for s in slots
        }
        self.z = [
            [
                links.add(place.to_z[1], acc(s, zs[1]), far_ref.at[s, 0], 2),
                links.add(place.to_z[1], acc(s, zs[3]), far_ref.at[s, 1], 2),
                links.add(place.to_z[2], mid_ref.at[s, 1], far_ref.at[s, 2], 2),
            ]
            for s in range(2)
        ]
        self.x = links.add(place.to_x, last_ref, side_ref, 2)

    def fold_y(self, s, half):
        for i, j in [(0, 1), (1, 3), (2, 2), (3, 0)][2 * half : 2 * half + 2]:
            z = self.place.zs[j]
            recv(self.y[s][i])
            value = self.work(s, z, self.place.y)[...].astype(F32)
            self.acc(s, z)[...] = (value + self.cross_ref[s, z].astype(F32)).astype(BF16)
            if i < 2:
                start(self.z[s][i])

    def fold_z(self, s):
        recv(self.z[s][:2])
        for i in (1, 0):
            value = self.acc(s, self.place.zs[2 * i])[...].astype(F32)
            self.mid_ref[s, i] = (value + self.far_ref[s, i].astype(F32)).astype(BF16)
            if i:
                start(self.z[s][2])

    def own(self, s):
        recv(self.z[s][2])
        return self.mid_ref[s, 0].astype(F32) + self.far_ref[s, 2].astype(F32)

    def send_x(self):
        self.last_ref[...] = self.own(1).astype(BF16)
        start(self.x)

    def total(self):
        value = self.own(0)
        recv(self.x)
        return value + self.side_ref[...].astype(F32)


def fused_backward(
    tokens_ref, gq_in, gw_in, rows_ref, dh1_ref, gb_ref, gbt_in, q_in, v_in, kt_in,
    p_ref, scale_in, o_in, a1t_in, layer_in, fold_in, work_in, early_ref,
    out_ref, layerout_ref, part0_ref, partw_ref, part1_ref, part2_ref, total_ref,
    gq_ref, gw_ref, q_ref, v_ref, kt_ref, scale_ref, o_ref,
    a1t_ref, gbt_ref, layer_ref, fold_ref, work_ref, do_ref, delta_ref, dkv_ref, dqkv_ref, da1_ref, own_ref, passing_ref, passlayer_ref, bqv_ref,
    folded_ref, cross1_ref, far1_ref, mid1_ref, last1_ref, side1_ref,
    cross2_ref, far2_ref, mid2_ref, last2_ref, side2_ref,
    stagew_ref, landw_ref, workw_ref, crossw_ref, farw_ref, midw_ref, lastw_ref, sidew_ref,
    stage0_ref, land0_ref, work0_ref, cross0_ref, far0_ref, mid0_ref, last0_ref, side0_ref,
    sums_ref, sumland_ref,
    send_sem, recv_sem, local_sem, result_sem, group_sem,
):
    t = pl.program_id(0)
    n = own_ref.shape[0]
    width = gw_ref.shape[-1]
    depth = part0_ref.shape[0]
    heads = width // HEAD_DIM
    step = n // 4
    place = Place()
    y = place.y
    links = Links(send_sem, recv_sem)
    k, i = group_and_block(t)
    mine = place.group(k)
    now = k % 2
    out = Result(links, place, own_ref, passing_ref, out_ref, step // 2, result_sem.at[0], 8)
    layer = Result(links, place, layer_ref, passlayer_ref, layerout_ref, step, result_sem.at[1], 3)
    fetch = pltpu.make_async_copy(tokens_ref.at[place.t], own_ref, local_sem.at[0])
    fetch_layer, fetch_work, fetch_fold, fetch_gbt, fetch_a1t = [
        pltpu.make_async_copy(there, here, local_sem.at[1 + j])
        for j, (there, here) in enumerate([
            (layer_in, layer_ref), (work_in, work_ref), (fold_in, fold_ref),
            (gbt_in, gbt_ref), (a1t_in, a1t_ref),
        ])
    ]
    def operands(group):
        slot = group % 2
        pairs = [
            (gw_in, gw_ref), (scale_in, scale_ref), (o_in, o_ref), (v_in, v_ref),
            (q_in, q_ref), (kt_in, kt_ref), (gq_in, gq_ref),
        ]
        return [
            pltpu.make_async_copy(there.at[group], here.at[slot], group_sem.at[slot, j])
            for j, (there, here) in enumerate(pairs)
        ]

    corew = [links.add(place.to_core, stagew_ref, landw_ref.at[i], Z_DEV) for i in range(2)]
    core0 = [links.add(place.to_core, stage0_ref, land0_ref.at[i], Z_DEV) for i in range(2)]
    def half_done(i, *landing):
        return Reduce(
            links, place, lambda s, z, y: work_ref.at[i, z, y],
            lambda s, z: folded_ref.at[i, z] if s else fold_ref.at[i, z],
            *landing, slots=(1,),
        )

    seg1 = half_done(0, cross1_ref, far1_ref, mid1_ref, last1_ref, side1_ref)
    seg2 = half_done(1, cross2_ref, far2_ref, mid2_ref, last2_ref, side2_ref)
    segw = Reduce(
        links, place, lambda s, z, y: workw_ref.at[s, z, y],
        lambda s, z: workw_ref.at[s, z, y],
        crossw_ref, farw_ref, midw_ref, lastw_ref, sidew_ref,
    )
    seg0 = Reduce(
        links, place, lambda s, z, y: work0_ref.at[s, z, y],
        lambda s, z: work0_ref.at[s, z, y],
        cross0_ref, far0_ref, mid0_ref, last0_ref, side0_ref,
    )
    sum_core, sum_y, *sum_z, sum_x = [
        links.add(to, sums_ref.at[i], sumland_ref.at[j])
        for j, (i, to) in enumerate(
            zip([0, 1, 2, 2, 2, 3], [place.to_core, place.to_y] + place.to_z[1:] + [place.to_x])
        )
    ]

    def when(point):
        return pl.when(t == point)

    @when(0)
    def _():
        start(fetch_layer, operands(1), fetch_work, fetch_fold, fetch_gbt, operands(0))
        start(fetch, fetch_a1t)
        place.greet()
        fetch_layer.wait()
        for i in range(3):
            layer.send(i)
        fetch_work.wait()
        start(seg1.y[1], seg2.y[1])
        fetch_fold.wait()
        start(seg1.z[0][:2], seg2.z[0][:2])
        bqv_ref[...] = jnp.zeros_like(bqv_ref)
        sums_ref[0] = early_ref[...]
        fetch_gbt.wait()

    def add_core():
        recv(corew[1])

        @pl.loop(0, Z_DEV)
        def _(z):
            workw_ref[1, z] = (
                workw_ref[1, z].astype(F32) + landw_ref[1, z].astype(F32)
            ).astype(BF16)

        start(segw.y[1])

    def wait(copies):
        for copy in copies:
            copy.wait()

    @when(0)
    def _():
        wait(operands(1))

    @when(4)
    def _():
        start(operands(3))
        wait(operands(0))

    @when(8)
    def _():
        start(operands(2))
        wait(operands(3))

    @when(9)
    def _():
        wait(operands(2))

    plan = [
        (2, 1, lambda: (seg1.fold_y(1, 0), seg1.fold_z(0))),
        (3, 1, lambda: layer.pass_on(0)),
        (4, 0, lambda: (seg1.fold_y(1, 1), seg2.fold_z(0))),
        (4, 1, lambda: layer.pass_on(1)),
        (5, 1, lambda: (seg1.fold_z(1), seg2.fold_y(1, 0))),
        (8, 0, lambda: (seg2.fold_y(1, 1), layer.pass_on(2))),
        (8, 1, lambda: (seg1.send_x(), segw.fold_y(0, 0), segw.fold_y(0, 1))),
        (9, 0, add_core),
        (9, 1, lambda: (seg2.fold_z(1), seg0.fold_y(0, 0))),
        (10, 1, lambda: segw.fold_z(0)),
        (11, 1, lambda: (seg2.send_x(), seg0.fold_y(0, 1))),
        (12, 1, lambda: (segw.fold_y(1, 0), segw.fold_y(1, 1))),
        (13, 1, lambda: (seg0.fold_z(0), (out.pass_on(7), out.pass_on(6)))),
        (14, 1, lambda: segw.fold_z(1)),
    ]

    def serve(point):
        for at, where, act in plan:
            if where == point:
                pl.when(t == at)(lambda act=act: (act(), None)[1])

    @pl.when((t == 0) | (t == 4) | (t == 8) | (t == 9))
    def _():
        pick = (
            lax.broadcasted_iota(jnp.int32, (8, width), 1) // HEAD_DIM
            == lax.broadcasted_iota(jnp.int32, (8, width), 0)
        ).astype(BF16)

        @pl.loop(0, n // step)
        def _(i):
            rows = pl.ds(pl.multiple_of(i * step, step), step)
            columns = scale_ref[now, :, rows].T
            lane = lax.broadcasted_iota(jnp.int32, (step, width), 1)
            scale = columns[:, heads - 1 : heads]
            for h in reversed(range(heads - 1)):
                scale = jnp.where(lane < (h + 1) * HEAD_DIM, columns[:, h : h + 1], scale)
            do = (dot_nn(gb_ref[rows, :], gw_ref[now]) * scale).astype(BF16)
            do_ref[now, rows, :] = do
            product = do.astype(F32) * o_ref[now, rows, :].astype(F32)
            high = product.astype(BF16)
            low = (product - high.astype(F32)).astype(BF16)
            delta_ref[now, :, rows] = dot_nt(pick, high) + dot_nt(pick, low)

        value = dot_nn(gbt_ref[...], o_ref[now]).reshape(Z_DEV, Y_DEV, depth, width)
        for s in range(2):
            @when(8 * s)
            def _():
                if s:
                    corew[0].wait_send()
                stagew_ref[...] = value.astype(BF16)
                start(corew[s])

        @when(4)
        def _():
            recv(corew[0])
            workw_ref[0] = (value + landw_ref[0].astype(F32)).astype(BF16)
            start(segw.y[0])

        @when(9)
        def _():
            workw_ref[1] = value.astype(BF16)

    serve(0)

    for ii in reversed(range(4)):
        @pl.when(i == ii)
        def _():
            first, last = ii * step, (ii + 1) * step
            do = do_ref[now, first:last, :]
            q = q_ref[now, first:last, :]
            v = v_ref[now, :last, :]
            lane = lax.broadcasted_iota(jnp.int32, (1, width), 1)
            dk, dv, dq = None, None, []
            for h in range(heads):
                low, high = h * HEAD_DIM, (h + 1) * HEAD_DIM
                here = (lane >= low) & (lane < high)
                p = p_ref[0, h, 0, :last, :]
                dp = dot_nt(v, jnp.where(here, do, jnp.zeros((), BF16)))
                ds = p * (dp - delta_ref[now, h : h + 1, first:last]).astype(BF16)
                part = dot_nn(p, do)
                dv = part if dv is None else jnp.where(lane < low, dv, part)
                part = dot_nn(ds, q)
                dk = part if dk is None else jnp.where(lane < low, dk, part)
                dq.append(dot_nn(kt_ref[now, low:high, :last], ds))
            if ii == 3:
                dkv_ref[now, 0] = dk
                dkv_ref[now, 1] = dv
            else:
                dkv_ref[now, 0, :last, :] += dk
                dkv_ref[now, 1, :last, :] += dv
            dk = dkv_ref[now, 0, first:last, :].astype(BF16)
            dv = dkv_ref[now, 1, first:last, :].astype(BF16)
            dq = (jnp.concatenate(dq, 0) * HEAD_DIM ** -0.5).astype(BF16).T
            dqkv_ref[now, first:last, :width] = dq
            dqkv_ref[now, first:last, width : 2 * width] = dk
            dqkv_ref[now, first:last, 2 * width :] = dv
            bqv_ref[mine, 0:1, :] += jnp.sum(dq.astype(F32), 0, keepdims=True)
            bqv_ref[mine, 1:2, :] += jnp.sum(dv.astype(F32), 0, keepdims=True)

            @pl.when(t >= 8)
            def _():
                da1_ref[first:last, :] += dot_nt(dqkv_ref[now, first:last, :], gq_ref[now])

    serve(1)

    @pl.when((t > 8) & (t % 2 == 1))
    def _():
        rows = pl.ds(pl.multiple_of(i * step, step), step)
        xhat, r = norm_parts(own_ref[rows, :].astype(F32))
        da1 = da1_ref[rows, :]
        sums_ref[0, 0:1, :] += jnp.sum(da1 * xhat, 0, keepdims=True)
        sums_ref[0, 2:3, :] += jnp.sum(da1, 0, keepdims=True)
        dg = da1 * rows_ref[0:1, :]
        dv = r * (
            dg
            - jnp.mean(dg, -1, keepdims=True)
            - xhat * jnp.mean(dg * xhat, -1, keepdims=True)
        )
        own_ref[rows, :] = (dh1_ref[...] + dv).astype(BF16)
        for ii in range(4):
            @pl.when(i == ii)
            def _():
                out.send(2 * ii + 1)
                out.send(2 * ii)

    @pl.when((t == 3) | (t == 7) | (t > 13))
    def _():
        @when(3)
        def _():
            fetch.wait()
            fetch_a1t.wait()

        @when(3)
        def _():
            da1_ref[...] = dot_nt(dqkv_ref[now], gq_ref[now])

        @when(7)
        def _():
            da1_ref[...] += dot_nt(dqkv_ref[now], gq_ref[now])

        value = dot_nn(a1t_ref[...], dqkv_ref[now]).reshape(Z_DEV, Y_DEV, depth, 3 * width)
        for s in range(2):
            @when(3 + 11 * s)
            def _():
                if s:
                    core0[0].wait_send()
                stage0_ref[...] = value.astype(BF16)
                start(core0[s])

            @when(7 + 8 * s)
            def _():
                recv(core0[s])
                work0_ref[s] = (value + land0_ref[s].astype(F32)).astype(BF16)
                start(seg0.y[s])

    @when(15)
    def _():
        for s in range(4):
            sums_ref[0, 3:5, s * width : (s + 1) * width] = bqv_ref[s, 0:2, :]
        start(sum_core)
        segw.send_x()
        out.pass_on(5)
        out.pass_on(4)
        recv(sum_core)
        sums_ref[1] = sums_ref[0] + sumland_ref[0]
        start(sum_y)
        seg0.fold_y(1, 0)
        out.pass_on(3)
        out.pass_on(2)
        seg0.fold_y(1, 1)
        recv(sum_y)
        sums_ref[2] = sums_ref[1] + sumland_ref[1]
        start(sum_z)
        seg0.fold_z(1)
        recv(sum_z)
        sums_ref[3] = (sums_ref[2] + sumland_ref[2]) + (sumland_ref[3] + sumland_ref[4])
        start(sum_x)
        part1_ref[...] = seg1.total()
        part2_ref[...] = seg2.total()
        seg0.send_x()
        partw_ref[...] = segw.total()
        layer.finish()
        out.pass_on(1)
        out.pass_on(0)
        recv(sum_x)
        total_ref[...] = sums_ref[3] + sumland_ref[5]
        part0_ref[...] = seg0.total()
        out.finish()
        links.sent(corew[0], core0[0])


def group_and_block(t):
    early = t < 8
    return (
        jnp.where(early, 1 - t // 4, 3 - t % 2),
        3 - jnp.where(early, t % 4, jnp.maximum(t - 8, 0) // 2),
    )


def run_fused_backward(
    tokens, gq, gw, rows, dh1, gb, gbt, q, v, kt, p, scale, o, a1t, layer, fold, work, early
):
    groups, n, _ = tokens.shape
    width = gw.shape[-1]
    heads = width // HEAD_DIM
    hidden = fold.shape[-1]
    depth = D // (Z_DEV * Y_DEV)
    step = n // 4

    p_spec = pl.BlockSpec(
        (1, heads, 1, n, step),
        lambda t: (group_and_block(t)[0], 0, group_and_block(t)[1], 0, 0),
    )

    copies = 24 + 9 + 4 + 2 * 15 + 2 * 11 + 6

    def landing(lanes):
        return [
            pltpu.VMEM((2, Z_DEV, depth, lanes), BF16),
            pltpu.VMEM((2, 3, depth, lanes), BF16), pltpu.VMEM((2, 2, depth, lanes), BF16),
            pltpu.VMEM((depth, lanes), BF16), pltpu.VMEM((depth, lanes), BF16),
        ]

    def working(lanes):
        block = (Z_DEV, Y_DEV, depth, lanes)
        return [pltpu.VMEM(block, BF16)] + [pltpu.VMEM((2,) + block, BF16)] * 2

    return pl.pallas_call(
        fused_backward,
        grid=(4 * groups,),
        in_specs=[
            ANY_WHOLE, ANY_WHOLE, ANY_WHOLE, VMEM_WHOLE,
            pl.BlockSpec((step, D), lambda t: (group_and_block(jnp.maximum(t, 8))[1], 0)),
            VMEM_WHOLE, ANY_WHOLE, ANY_WHOLE, ANY_WHOLE, ANY_WHOLE, p_spec,
            ANY_WHOLE, ANY_WHOLE, ANY_WHOLE, ANY_WHOLE, ANY_WHOLE, ANY_WHOLE, VMEM_WHOLE,
        ],
        out_specs=[ANY_WHOLE] * 2 + [VMEM_WHOLE] * 5,
        out_shape=[
            shaped(BF16, groups, n, D), shaped(BF16, groups, n - step, D),
            shaped(F32, depth, 3 * width),
            shaped(F32, depth, width), shaped(F32, depth, hidden),
            shaped(F32, depth, hidden), shaped(F32, 16, D),
        ],
        scratch_shapes=[
            pltpu.VMEM((2, D, 3 * width), BF16), pltpu.VMEM((2, D, width), BF16),
            pltpu.VMEM((2, n, width), BF16), pltpu.VMEM((2, n, width), BF16),
            pltpu.VMEM((2, width, n), BF16), pltpu.VMEM((2, 8, n), F32),
            pltpu.VMEM((2, n, width), BF16),
            pltpu.VMEM((D, n), BF16), pltpu.VMEM((D, n), BF16), pltpu.VMEM((n - step, D), BF16),
            pltpu.VMEM((2, Z_DEV, depth, hidden), BF16),
            pltpu.VMEM((2, Z_DEV, Y_DEV, depth, hidden), BF16),
            pltpu.VMEM((2, n, width), BF16),
            pltpu.VMEM((2, 8, n), F32), pltpu.VMEM((2, 2, n, width), F32),
            pltpu.VMEM((2, n, 3 * width), BF16), pltpu.VMEM((n, D), F32),
            pltpu.VMEM((n, D), BF16), pltpu.VMEM((n, D), BF16), pltpu.VMEM((n - step, D), BF16),
            pltpu.VMEM((groups, 8, width), F32),
        ]
        + landing(hidden)[:1] + landing(hidden) + landing(hidden)
        + working(width) + landing(width)
        + working(3 * width) + landing(3 * width)
        + [
            pltpu.VMEM((4, 16, D), F32), pltpu.VMEM((6, 16, D), F32),
            pltpu.SemaphoreType.DMA((copies,)), pltpu.SemaphoreType.DMA((copies,)),
            pltpu.SemaphoreType.DMA((6,)), pltpu.SemaphoreType.DMA((2, 2, 8)),
            pltpu.SemaphoreType.DMA((2, 7)),
        ],
        compiler_params=pltpu.CompilerParams(
            vmem_limit_bytes=VMEM_LIMIT, collective_id=2, has_side_effects=True
        ),
        name="fused_backward",
    )(tokens, gq, gw, rows, dh1, gb, gbt, q, v, kt, p, scale, o, a1t, layer, fold, work, early)


def place_gradients(
    tie_ref, sums_ref, part0_ref, partw_ref, part1_ref, part2_ref, near_out_ref, near_rest_ref,
    near_grad_ref, far_out_ref, far_grad_ref, gains_ref, bias_ref, in_ref, out_ref, expand_ref,
    project_ref,
):
    first = near_out_ref.shape[1]
    far_out_ref[0, :first] = near_out_ref[0]
    far_out_ref[0, first:] = near_rest_ref[0]
    far_grad_ref[...] = near_grad_ref[...]
    own = gains_ref.shape[-1]
    width = partw_ref.shape[-1]

    @pl.when(pl.program_id(0) == 0)
    def _():
        origin = (lax.axis_index("dp") * 4 + lax.axis_index("tensor")) * own
        feature = lax.broadcasted_iota(jnp.int32, (D, 128), 0)
        lane = lax.broadcasted_iota(jnp.int32, (D, 128), 1)
        chosen = ((feature == origin + lane) & (lane < own)).astype(F32)
        sums = lax.dot_general(
            sums_ref[...], chosen, (((1,), (0,)), ((), ())),
            precision=lax.Precision.HIGHEST, preferred_element_type=F32,
        )[:, :own]
        s0, s1, s2, s3 = tie_ref[0], tie_ref[1], tie_ref[2], tie_ref[3]
        w_out = partw_ref[...].T

        def at(source, wanted, value):
            return jnp.where(source == wanted, value, jnp.zeros_like(value))

        row = lax.broadcasted_iota(jnp.int32, (NSRC, own), 0)
        for i, wanted in enumerate([s0, s0, s0, s1, s2, s3, s2, s2, s2, s2]):
            bias_ref[i] = jnp.where(row == wanted, sums[2 + i : 3 + i], 0.0)
        for s in range(NSRC):
            gains_ref[s, 0:1] = at(s, s0, sums[0:1])
            gains_ref[s, 1:2] = at(s, s2, sums[1:2])
            for j in range(3):
                in_ref[s, j] = at(s, s0, part0_ref[:, j * width : (j + 1) * width])
            out_ref[s] = at(s, s1, w_out)
            expand_ref[s] = at(s, s2, part1_ref[...])
            project_ref[s] = at(s, s3, part2_ref[...])


def run_place_gradients(tie, sums, part0, partw, part1, part2, out, rest, grad, like):
    slots, n, _ = grad.shape
    gains, biases, w_in, w_out, w_expand, w_project = [item.shape for item in like]
    shapes = [
        gains, (biases[1], biases[0], biases[2]), w_in, w_out, w_expand,
        (w_project[0], w_project[2], w_project[1]),
    ]
    out, grad, gains, biases, w_in, w_out, w_expand, w_project = pl.pallas_call(
        place_gradients,
        grid=(slots,),
        in_specs=[SMEM_WHOLE] + [VMEM_WHOLE] * 5
        + [group(n // 4, D), group(n - n // 4, D), group(n, D)],
        out_specs=[group(n, D), group(n, D)] + [VMEM_WHOLE] * 6,
        out_shape=[shaped(BF16, slots, n, D)] * 2 + [shaped(F32, *item) for item in shapes],
        compiler_params=pltpu.CompilerParams(vmem_limit_bytes=VMEM_LIMIT),
        name="place_gradients",
    )(tie, sums, part0, partw, part1, part2, out, rest, grad)
    biases = biases.transpose(1, 0, 2)
    return out, grad, gains, biases, w_in, w_out, w_expand, w_project.transpose(0, 2, 1)


def plain_step(
    tokens, lengths, tie_map, norm_gains, bias_rows, attention_in, attention_out,
    expand_weight, project_weight, cotangent,
):
    slot_rows = tokens.shape[0] // lengths.shape[0]
    me = lax.axis_index("tensor")
    in_local = lax.dynamic_index_in_dim(attention_in, tie_map[0], 0, keepdims=False)
    out_local = lax.dynamic_index_in_dim(attention_out, tie_map[1], 0, keepdims=False)
    expand_local = lax.dynamic_index_in_dim(expand_weight, tie_map[2], 0, keepdims=False)
    project_local = lax.dynamic_index_in_dim(project_weight, tie_map[3], 0, keepdims=False)
    local0 = jnp.concatenate([in_local, out_local.T[None]], 0)
    row_kinds = jnp.array([0, 0, 0, 1, 2, 3] + [2] * (FF // D), dtype=jnp.int32)
    gain_kinds = jnp.array([0, 2], dtype=jnp.int32)
    gain_pick = norm_gains[tie_map[gain_kinds], jnp.arange(2)]
    bias_pick = bias_rows[tie_map[row_kinds], jnp.arange(row_kinds.shape[0])]
    vectors = jnp.concatenate([gain_pick, bias_pick], 0)
    x = lax.dynamic_slice_in_dim(tokens, me * slot_rows, slot_rows, 0)
    cot = lax.dynamic_slice_in_dim(cotangent, me * slot_rows, slot_rows, 0)
    length = lax.dynamic_slice_in_dim(lengths, me, 1, 0)
    rows = lax.all_gather(vectors, ("dp", "tensor"), axis=1, tiled=True).astype(F32)
    rows = jnp.concatenate([rows, jnp.zeros((4, D), F32)], 0)

    def gathered(piece, axis):
        piece = lax.all_gather(piece, "dp", axis=axis, tiled=True)
        return lax.all_gather(piece, "tensor", axis=0)

    g0 = gathered(local0, 1)
    g1 = gathered(expand_local, 0)
    g2 = gathered(project_local.T, 0)
    groups, width = g0.shape[0], g0.shape[-1]
    bqv = rows[3:5].reshape(2, groups, width).transpose(1, 0, 2)
    q, v, kt, p, o, a1t, h1, a2, a2t = run_attention_forward(length, x, g0, rows, bqv)
    out, d1, d2, dh1, gb, gbt, sums = run_feed_forward(length, cot, a2, a2t, h1, g1, g2, rows)
    d0, xg, sums_in, sums_qv = run_attention_backward(
        x, g0, rows, dh1, gb, gbt, q, v, kt, p, o, a1t
    )
    layer_out = lax.all_gather(out, "tensor", axis=0, tiled=True)
    tokens_grad = lax.all_gather(xg, "tensor", axis=0, tiled=True)

    def scattered(piece, axis):
        piece = lax.psum_scatter(piece, "tensor", scatter_dimension=0)
        return lax.psum_scatter(piece, "dp", scatter_dimension=axis, tiled=True).astype(F32)

    part0 = scattered(d0, 1)
    part1 = scattered(d1, 0)
    part2 = scattered(d2, 0)
    qv = sums_qv[:, :2].transpose(1, 0, 2).reshape(2, D)
    sums = jnp.concatenate(
        [sums_in[0:1], sums[1:2], sums_in[1:2], qv, sums[5:12]], 0
    )
    sums = lax.psum_scatter(sums, ("dp", "tensor"), scatter_dimension=1, tiled=True)
    return layer_out, tokens_grad, *placed(tie_map, sums, part0, part1, part2)


def fused_step(
    tokens, lengths, tie_map, norm_gains, bias_rows, attention_in, attention_out,
    expand_weight, project_weight, cotangent,
):
    slots = lengths.shape[0]
    tokens = tokens.reshape(slots, -1, D)
    cotangent = cotangent.reshape(slots, -1, D)
    gq, gw, g1, g2, rows, q, v, kt, p, scale, o, a1t, h1, a2, a2t = run_fused_forward(
        tie_map, lengths, tokens, norm_gains, bias_rows, attention_in, attention_out,
        expand_weight, project_weight,
    )
    out, layer, fold, work, dh1, gb, gbt, early = run_fused_feed_forward(
        lengths, cotangent, a2, a2t, h1, g1, g2, rows
    )
    grad, rest, part0, partw, part1, part2, sums = run_fused_backward(
        tokens, gq, gw, rows, dh1, gb, gbt, q, v, kt, p, scale, o, a1t, layer, fold,
        work, early,
    )
    out, grad, *placed_grads = run_place_gradients(
        tie_map, sums, part0, partw, part1, part2, out, rest, grad,
        (norm_gains, bias_rows, attention_in, attention_out, expand_weight, project_weight),
    )
    return out.reshape(-1, D), grad.reshape(-1, D), *placed_grads


def placed(tie_map, sums, part0, part1, part2):
    source = jnp.arange(NSRC, dtype=jnp.int32)

    def place(piece, which):
        pick = (source == tie_map[which]).reshape((NSRC,) + (1,) * piece.ndim)
        return jnp.where(pick, piece[None], 0.0)

    def place_rows(piece, kinds):
        pick = source[:, None] == tie_map[jnp.array(kinds, dtype=jnp.int32)][None, :]
        return jnp.where(pick[:, :, None], piece[None], 0.0)

    return (
        place_rows(sums[:2], [0, 2]),
        place_rows(sums[2:], [0, 0, 0, 1, 2, 3] + [2] * (FF // D)),
        place(part0[:3], 0),
        place(part0[3].T, 1),
        place(part1, 2),
        place(part2.T, 3),
    )


def solution(mesh):
    fused = mesh.shape["dp"] == Z_DEV * Y_DEV and mesh.shape["tensor"] == X_DEV * C_DEV
    return jax.shard_map(
        fused_step if fused else plain_step,
        mesh=mesh,
        in_specs=(
            P("dp", None),
            P("dp"),
            P(),
            P(None, None, ("dp", "tensor")),
            P(None, None, ("dp", "tensor")),
            P(None, None, "dp", "tensor"),
            P(None, "tensor", "dp"),
            P(None, "dp", "tensor"),
            P(None, "tensor", "dp"),
            P("dp", None),
        ),
        out_specs=(
            P("dp", None),
            P("dp", None),
            P(None, None, ("dp", "tensor")),
            P(None, None, ("dp", "tensor")),
            P(None, None, "dp", "tensor"),
            P(None, "tensor", "dp"),
            P(None, "dp", "tensor"),
            P(None, "tensor", "dp"),
        ),
        check_vma=False,
    )
```

```python
import jax
import jax.numpy as jnp
from jax import lax
from jax.experimental import pallas as pl
from jax.experimental.pallas import tpu as pltpu
from jax.sharding import PartitionSpec as P

D = 768
HEAD_DIM = 64
FF = 3072
NSRC = 4
EPS = 1e-05
MASKED = -1e30
F32 = jnp.float32
BF16 = jnp.bfloat16
VMEM_LIMIT = 60 * 1024 * 1024


def dot_nn(a, b):
    return lax.dot_general(a, b, (((1,), (0,)), ((), ())), preferred_element_type=F32)


def dot_nt(a, b):
    return lax.dot_general(a, b, (((1,), (1,)), ((), ())), preferred_element_type=F32)


def norm_parts(v):
    center = jnp.mean(v, -1, keepdims=True)
    centered = v - center
    r = lax.rsqrt(jnp.mean(centered * centered, -1, keepdims=True) + EPS)
    return centered * r, r


def head_mask(shape, h):
    lane = lax.broadcasted_iota(jnp.int32, shape, 1)
    return (lane >= h * HEAD_DIM) & (lane < (h + 1) * HEAD_DIM)


def blocks(total, size):
    return [slice(i * size, (i + 1) * size) for i in range(total // size)]


def attention_forward(
    len_ref, x_ref, g_ref, rows_ref, bqv_ref,
    q_ref, v_ref, kt_ref, p_ref, o_ref, a1t_ref, h1_ref, a2_ref, a2t_ref,
    a1_ref, k_ref, vt_ref, ot_ref, attn_ref,
):
    t = pl.program_id(0)
    n = x_ref.shape[0]
    width = g_ref.shape[-1]
    heads = width // HEAD_DIM
    step = 256
    length = len_ref[0]

    @pl.when(t == 0)
    def _():
        @pl.loop(0, n // step)
        def _(b):
            rows = pl.ds(pl.multiple_of(b * step, step), step)
            xhat, _ = norm_parts(x_ref[rows, :].astype(F32))
            a1 = xhat * rows_ref[0:1, :] + rows_ref[2:3, :]
            a1_ref[rows, :] = a1.astype(BF16)
            a1t_ref[:, rows] = a1.astype(BF16).T
            attn_ref[rows, :] = x_ref[rows, :].astype(F32) + rows_ref[5:6, :]

    @pl.loop(0, n // step)
    def _(b):
        rows = pl.ds(pl.multiple_of(b * step, step), step)
        a1 = a1_ref[rows, :]
        q = (dot_nn(a1, g_ref[0, 0]) + bqv_ref[0, 0:1, :]).astype(BF16)
        q_ref[0, rows, :] = q * jnp.asarray(HEAD_DIM ** -0.5, BF16)
        k = dot_nn(a1, g_ref[0, 1]).astype(BF16)
        k_ref[rows, :] = k
        kt_ref[0, :, rows] = k.T
        v = (dot_nn(a1, g_ref[0, 2]) + bqv_ref[0, 1:2, :]).astype(BF16)
        v_ref[0, rows, :] = v
        vt_ref[:, rows] = v.T

    for h in range(heads):
        k = k_ref[...]
        k = jnp.where(head_mask(k.shape, h), k, jnp.zeros_like(k))
        for b in range(n // step):
            first, last = b * step, (b + 1) * step
            q = q_ref[0, first:last, :]
            key = lax.broadcasted_iota(jnp.int32, (last, step), 0)
            query = lax.broadcasted_iota(jnp.int32, (step, step), 1) + first
            s = dot_nt(k[:last], q)
            near = jnp.where(
                (key[first:] <= query) & (key[first:] < length), s[first:], MASKED
            )
            if b:
                far = jnp.where(key[:first] < length, s[:first], MASKED)
                top = jnp.maximum(
                    jnp.max(far, 0, keepdims=True), jnp.max(near, 0, keepdims=True)
                )
                e_far = jnp.exp(far - top)
                e_near = jnp.exp(near - top)
                total = jnp.sum(e_far, 0, keepdims=True) + jnp.sum(e_near, 0, keepdims=True)
                scale = 1.0 / total
                p_ref[0, h, :first, first:last] = (e_far * scale).astype(BF16)
            else:
                top = jnp.max(near, 0, keepdims=True)
                e_near = jnp.exp(near - top)
                scale = 1.0 / jnp.sum(e_near, 0, keepdims=True)
            p_ref[0, h, first:last, first:last] = (e_near * scale).astype(BF16)
            ot_ref[h * HEAD_DIM : (h + 1) * HEAD_DIM, first:last] = dot_nn(
                vt_ref[h * HEAD_DIM : (h + 1) * HEAD_DIM, :last],
                p_ref[0, h, :last, first:last],
            ).astype(BF16)

    @pl.loop(0, n // step)
    def _(b):
        rows = pl.ds(pl.multiple_of(b * step, step), step)
        o = ot_ref[:, rows].T
        o_ref[0, rows, :] = o
        attn_ref[rows, :] += dot_nt(o, g_ref[0, 3])

    @pl.when(t == pl.num_programs(0) - 1)
    def _():
        @pl.loop(0, n // step)
        def _(b):
            rows = pl.ds(pl.multiple_of(b * step, step), step)
            h1 = attn_ref[rows, :]
            h1_ref[rows, :] = h1
            xhat, _ = norm_parts(h1)
            a2 = (xhat * rows_ref[1:2, :] + rows_ref[6:7, :]).astype(BF16)
            a2_ref[rows, :] = a2
            a2t_ref[:, rows] = a2.T


SQRT_2_PI = 0.7978845608028654


def feed_forward_both(
    len_ref, c_ref, a2_ref, a2t_ref, h1_ref, w1_ref, w2_ref, rows_ref,
    out_ref, d1_ref, d2_ref, dh1_ref, gb_ref, gbt_ref, sums_ref,
    gf_ref, gft_ref, feed_ref, da2_ref, h_ref, df_ref,
):
    t = pl.program_id(0)
    n = c_ref.shape[0]
    step = 256
    length = len_ref[0]

    @pl.when(t == 0)
    def _():
        sums_ref[...] = jnp.zeros_like(sums_ref)

        @pl.loop(0, n // step)
        def _(b):
            rows = pl.ds(pl.multiple_of(b * step, step), step)
            place = b * step + lax.broadcasted_iota(jnp.int32, (step, 1), 0)
            live = (place < length).astype(F32)
            g = (c_ref[rows, :].astype(F32) * live).astype(BF16)
            gf_ref[rows, :] = g
            gft_ref[:, rows] = g.T
            sums_ref[7:8, :] += jnp.sum(g.astype(F32), 0, keepdims=True)

    bias = rows_ref[pl.ds(8 + t, 1), :]

    @pl.loop(0, n // step)
    def _(b):
        rows = pl.ds(pl.multiple_of(b * step, step), step)
        f = dot_nn(a2_ref[rows, :], w1_ref[0]) + bias
        dh = dot_nn(gf_ref[rows, :], w2_ref[0])
        f2 = f * f
        th = jnp.tanh(f * (SQRT_2_PI + (SQRT_2_PI * 0.044715) * f2))
        half = 0.5 + 0.5 * th
        h = (f * half).astype(BF16)
        slope = half + f * (0.5 - 0.5 * th * th) * (
            SQRT_2_PI + (3 * SQRT_2_PI * 0.044715) * f2
        )
        df = (dh * slope).astype(BF16)
        h_ref[rows, :] = h
        df_ref[rows, :] = df
        sums_ref[pl.ds(8 + t, 1), :] += jnp.sum(df.astype(F32), 0, keepdims=True)
        feed = dot_nt(h, w2_ref[0])
        da2 = dot_nt(df, w1_ref[0])

        @pl.when(t == 0)
        def _():
            feed_ref[rows, :] = feed
            da2_ref[rows, :] = da2

        @pl.when(t > 0)
        def _():
            feed_ref[rows, :] += feed
            da2_ref[rows, :] += da2

    @pl.loop(0, D // step)
    def _(b):
        rows = pl.ds(pl.multiple_of(b * step, step), step)
        d1_ref[0, rows, :] = dot_nn(a2t_ref[rows, :], df_ref[...]).astype(BF16)
        d2_ref[0, rows, :] = dot_nn(gft_ref[rows, :], h_ref[...]).astype(BF16)

    @pl.when(t == pl.num_programs(0) - 1)
    def _():
        @pl.loop(0, n // step)
        def _(b):
            rows = pl.ds(pl.multiple_of(b * step, step), step)
            place = b * step + lax.broadcasted_iota(jnp.int32, (step, 1), 0)
            live = (place < length).astype(F32)
            h1 = h1_ref[rows, :]
            out_ref[rows, :] = (live * (h1 + (feed_ref[rows, :] + rows_ref[7:8, :]))).astype(BF16)
            xhat, r = norm_parts(h1)
            da2 = da2_ref[rows, :]
            sums_ref[1:2, :] += jnp.sum(da2 * xhat, 0, keepdims=True)
            sums_ref[6:7, :] += jnp.sum(da2, 0, keepdims=True)
            dg = da2 * rows_ref[1:2, :]
            dv = r * (
                dg
                - jnp.mean(dg, -1, keepdims=True)
                - xhat * jnp.mean(dg * xhat, -1, keepdims=True)
            )
            dh1 = live * c_ref[rows, :].astype(F32) + dv
            dh1_ref[rows, :] = dh1
            gb = dh1.astype(BF16)
            gb_ref[rows, :] = gb
            gbt_ref[:, rows] = gb.T
            sums_ref[5:6, :] += jnp.sum(gb.astype(F32), 0, keepdims=True)


def attention_backward(
    x_ref, g_ref, rows_ref, dh1_ref, gb_ref, gbt_ref, q_ref, v_ref, kt_ref, p_ref,
    o_ref, a1t_ref,
    d0_ref, xg_ref, sums_ref, bqv_ref,
    do_ref, delta_ref, dqt_ref, dq_ref, dk_ref, dv_ref, da1_ref,
):
    t = pl.program_id(0)
    n = x_ref.shape[0]
    width = g_ref.shape[-1]
    heads = width // HEAD_DIM
    step = 256
    pick = (
        lax.broadcasted_iota(jnp.int32, (16, width), 1) // HEAD_DIM
        == lax.broadcasted_iota(jnp.int32, (16, width), 0)
    ).astype(BF16)

    @pl.loop(0, n // step)
    def _(b):
        rows = pl.ds(pl.multiple_of(b * step, step), step)
        do = dot_nn(gb_ref[rows, :], g_ref[0, 3]).astype(BF16)
        do_ref[rows, :] = do
        prod = do.astype(F32) * o_ref[0, rows, :].astype(F32)
        high = prod.astype(BF16)
        low = (prod - high.astype(F32)).astype(BF16)
        delta_ref[:, rows] = dot_nt(pick, high) + dot_nt(pick, low)

    dqt_ref[...] = jnp.zeros_like(dqt_ref)
    for b in range(n // step):
        first, last = b * step, (b + 1) * step
        do = do_ref[first:, :]
        q = q_ref[0, first:, :]
        v = v_ref[0, first:last, :]
        dk, dv = None, None
        for h in range(heads):
            mine = head_mask((1, width), h)
            zero = jnp.zeros((), BF16)
            p = p_ref[0, h, first:last, first:]
            dp = dot_nt(jnp.where(mine, v, zero), do)
            ds = (p.astype(F32) * (dp - delta_ref[h : h + 1, first:])).astype(BF16)
            part = dot_nn(p, jnp.where(mine, do, zero))
            dv = part if dv is None else dv + part
            part = dot_nn(ds, jnp.where(mine, q, zero))
            dk = part if dk is None else dk + part
            head = slice(h * HEAD_DIM, (h + 1) * HEAD_DIM)
            dqt_ref[head, first:] += dot_nn(kt_ref[0, head, first:last], ds)
        dk_ref[first:last, :] = dk.astype(BF16)
        dv_ref[first:last, :] = dv.astype(BF16)

    @pl.when(t == 0)
    def _():
        da1_ref[...] = jnp.zeros_like(da1_ref)

    bqv_ref[...] = jnp.zeros_like(bqv_ref)

    @pl.loop(0, n // step)
    def _(b):
        rows = pl.ds(pl.multiple_of(b * step, step), step)
        dq = (dqt_ref[:, rows] * HEAD_DIM ** -0.5).astype(BF16).T
        dk = dk_ref[rows, :]
        dv = dv_ref[rows, :]
        dq_ref[rows, :] = dq
        bqv_ref[0, 0:1, :] += jnp.sum(dq.astype(F32), 0, keepdims=True)
        bqv_ref[0, 1:2, :] += jnp.sum(dv.astype(F32), 0, keepdims=True)
        da1_ref[rows, :] += (
            dot_nt(dq, g_ref[0, 0]) + dot_nt(dk, g_ref[0, 1]) + dot_nt(dv, g_ref[0, 2])
        )

    @pl.loop(0, D // step)
    def _(b):
        rows = pl.ds(pl.multiple_of(b * step, step), step)
        a1t = a1t_ref[rows, :]
        d0_ref[0, 0, rows, :] = dot_nn(a1t, dq_ref[...]).astype(BF16)
        d0_ref[0, 1, rows, :] = dot_nn(a1t, dk_ref[...]).astype(BF16)
        d0_ref[0, 2, rows, :] = dot_nn(a1t, dv_ref[...]).astype(BF16)
        d0_ref[0, 3, rows, :] = dot_nn(gbt_ref[rows, :], o_ref[0]).astype(BF16)

    @pl.when(t == pl.num_programs(0) - 1)
    def _():
        sums_ref[...] = jnp.zeros_like(sums_ref)

        @pl.loop(0, n // step)
        def _(b):
            rows = pl.ds(pl.multiple_of(b * step, step), step)
            xhat, r = norm_parts(x_ref[rows, :].astype(F32))
            da1 = da1_ref[rows, :]
            sums_ref[0:1, :] += jnp.sum(da1 * xhat, 0, keepdims=True)
            sums_ref[1:2, :] += jnp.sum(da1, 0, keepdims=True)
            dg = da1 * rows_ref[0:1, :]
            dv = r * (
                dg
                - jnp.mean(dg, -1, keepdims=True)
                - xhat * jnp.mean(dg * xhat, -1, keepdims=True)
            )
            xg_ref[rows, :] = (dh1_ref[rows, :] + dv).astype(BF16)


def whole(*shape):
    return pl.BlockSpec(shape, lambda t: (0,) * len(shape))


def group(*shape):
    return pl.BlockSpec((1,) + shape, lambda t: (t,) + (0,) * len(shape))


def shaped(dtype, *shape):
    return jax.ShapeDtypeStruct(shape, dtype)


SMEM_WHOLE = pl.BlockSpec(memory_space=pltpu.SMEM)


def run_attention_forward(length, x, g0, rows, bqv):
    n = x.shape[0]
    groups, _, _, width = g0.shape
    heads = width // HEAD_DIM
    return pl.pallas_call(
        attention_forward,
        grid=(groups,),
        in_specs=[SMEM_WHOLE, whole(n, D), group(4, D, width), whole(16, D), group(2, width)],
        out_specs=[
            group(n, width), group(n, width), group(width, n), group(heads, n, n),
            group(n, width), whole(D, n), whole(n, D), whole(n, D), whole(D, n),
        ],
        out_shape=[
            shaped(BF16, groups, n, width), shaped(BF16, groups, n, width),
            shaped(BF16, groups, width, n), shaped(BF16, groups, heads, n, n),
            shaped(BF16, groups, n, width), shaped(BF16, D, n), shaped(F32, n, D),
            shaped(BF16, n, D), shaped(BF16, D, n),
        ],
        scratch_shapes=[
            pltpu.VMEM((n, D), BF16), pltpu.VMEM((n, width), BF16),
            pltpu.VMEM((width, n), BF16), pltpu.VMEM((width, n), BF16),
            pltpu.VMEM((n, D), F32),
        ],
        compiler_params=pltpu.CompilerParams(vmem_limit_bytes=VMEM_LIMIT),
        name="attention_forward",
    )(length, x, g0, rows, bqv)


def run_feed_forward(length, cot, a2, a2t, h1, g1, g2, rows):
    n = cot.shape[0]
    groups, _, width = g1.shape
    return pl.pallas_call(
        feed_forward_both,
        grid=(groups,),
        in_specs=[
            SMEM_WHOLE, whole(n, D), whole(n, D), whole(D, n), whole(n, D),
            group(D, width), group(D, width), whole(16, D),
        ],
        out_specs=[
            whole(n, D), group(D, width), group(D, width), whole(n, D), whole(n, D),
            whole(D, n), whole(16, D),
        ],
        out_shape=[
            shaped(BF16, n, D), shaped(BF16, groups, D, width), shaped(BF16, groups, D, width),
            shaped(F32, n, D), shaped(BF16, n, D), shaped(BF16, D, n), shaped(F32, 16, D),
        ],
        scratch_shapes=[
            pltpu.VMEM((n, D), BF16), pltpu.VMEM((D, n), BF16), pltpu.VMEM((n, D), F32),
            pltpu.VMEM((n, D), F32), pltpu.VMEM((n, width), BF16), pltpu.VMEM((n, width), BF16),
        ],
        compiler_params=pltpu.CompilerParams(vmem_limit_bytes=VMEM_LIMIT),
        name="feed_forward_both",
    )(length, cot, a2, a2t, h1, g1, g2, rows)


def run_attention_backward(x, g0, rows, dh1, gb, gbt, q, v, kt, p, o, a1t):
    n = x.shape[0]
    groups, _, _, width = g0.shape
    heads = width // HEAD_DIM
    return pl.pallas_call(
        attention_backward,
        grid=(groups,),
        in_specs=[
            whole(n, D), group(4, D, width), whole(16, D), whole(n, D), whole(n, D),
            whole(D, n), group(n, width), group(n, width), group(width, n),
            group(heads, n, n), group(n, width), whole(D, n),
        ],
        out_specs=[group(4, D, width), whole(n, D), whole(8, D), group(8, width)],
        out_shape=[
            shaped(BF16, groups, 4, D, width), shaped(BF16, n, D), shaped(F32, 8, D),
            shaped(F32, groups, 8, width),
        ],
        scratch_shapes=[
            pltpu.VMEM((n, width), BF16), pltpu.VMEM((16, n), F32), pltpu.VMEM((width, n), F32),
            pltpu.VMEM((n, width), BF16), pltpu.VMEM((n, width), BF16),
            pltpu.VMEM((n, width), BF16), pltpu.VMEM((n, D), F32),
        ],
        compiler_params=pltpu.CompilerParams(vmem_limit_bytes=VMEM_LIMIT),
        name="attention_backward",
    )(x, g0, rows, dh1, gb, gbt, q, v, kt, p, o, a1t)


Z_DEV, Y_DEV, X_DEV, C_DEV = 4, 2, 2, 2


class Place:
    def __init__(self):
        dp, self.t = lax.axis_index("dp"), lax.axis_index("tensor")
        self.dp = dp
        self.z, self.y = dp // 2, dp % 2
        self.x, self.c = self.t // 2, self.t % 2
        self.other_y = 1 - self.y
        self.zs = [
            self.z,
            self.z + 1 - 2 * (self.z % 2),
            self.z + 2 - 4 * (self.z // 2),
            3 - self.z,
        ]
        self.ts = [
            self.t,
            self.t + 1 - 2 * (self.t % 2),
            self.t + 2 - 4 * (self.t // 2),
            3 - self.t,
        ]
        self.to_z = [dict(dp=z * 2 + self.y) for z in self.zs]
        self.to_y = dict(dp=self.z * 2 + self.other_y)
        self.to_x = dict(tensor=self.ts[2])
        self.same_t = self.to_z[1:] + [dict(dp=z * 2 + self.other_y) for z in self.zs]
        self.same_dp = [dict(tensor=t) for t in self.ts[1:]]
        self.to_core = dict(tensor=self.ts[1])

    def group(self, k):
        return lax.select(
            k == 0, self.ts[0],
            lax.select(k == 1, self.ts[1], lax.select(k == 2, self.ts[2], self.ts[3])),
        )

    def greet(self, others=None):
        barrier = pltpu.get_barrier_semaphore()
        others = others or self.to_z[1:] + [self.to_y, self.to_x, self.to_core]
        for device in others:
            pl.semaphore_signal(
                barrier, inc=1, device_id=device, device_id_type=pl.DeviceIdType.MESH
            )
        pl.semaphore_wait(barrier, len(others))


class Pieces:
    def __init__(self, whole, pieces):
        self.whole, self.pieces = whole, pieces

    def start(self):
        for piece in self.pieces:
            piece.start()

    def wait_recv(self):
        self.whole.wait_recv()

    def wait_send(self):
        self.whole.wait_send()


class Links:
    def __init__(self, send_sem, recv_sem):
        self.send_sem, self.recv_sem = send_sem, recv_sem
        self.copies = []

    def add(self, device, src, dst, parts=1, axis=0):
        number = len(self.copies)

        def make(src, dst):
            return pltpu.make_async_remote_copy(
                src_ref=src,
                dst_ref=dst,
                send_sem=self.send_sem.at[number],
                recv_sem=self.recv_sem.at[number],
                device_id=device,
                device_id_type=pl.DeviceIdType.MESH,
            )

        size = src.shape[axis] // parts
        cuts = [(slice(None),) * axis + (pl.ds(i * size, size),) for i in range(parts)]
        copy = Pieces(make(src, dst), [make(src.at[cut], dst.at[cut]) for cut in cuts])
        self.copies.append(copy)
        return copy

    def sent(self, *apart):
        for copy in self.copies:
            if all(copy is not other for other in apart):
                copy.wait_send()


def flat(copies):
    for item in copies:
        if isinstance(item, list):
            yield from flat(item)
        else:
            yield item


def start(*copies):
    for copy in flat(copies):
        copy.start()


def weave(*copies):
    rows = [copy.pieces for copy in flat(copies)]
    for i in range(max(len(row) for row in rows)):
        for row in rows:
            if i < len(row):
                row[i].start()


def recv(*copies):
    for copy in flat(copies):
        copy.wait_recv()


class Gather:
    def __init__(self, links, place, own, full, order, single=True, last=True):
        every = slice(None)
        y, other = place.y, place.other_y

        def same(device, k, yy, to):
            return links.add(device, full(k, every, yy), full(to, every, yy), Z_DEV)

        def along_z(k, yy, block):
            here, passed = full(k, place.z, yy), full(k, place.zs[2], yy)
            return [
                links.add(place.to_z[1], block, here, 2),
                links.add(place.to_z[2], block, here, 2),
                links.add(place.to_z[1], passed, passed, 2),
            ]

        self.z = along_z(0, y, own)
        if order == X_Z_Y:
            self.first = [links.add(place.to_x, own, full(2, place.z, y), 2)]
            self.far = along_z(2, y, full(2, place.z, y))
            blocks = [(0, y), (2, y), (0, other), (2, other)]
        else:
            blocks = [(0, y), (0, other), (2, y), (2, other)]
        if order == Y_Z_X:
            self.first = [links.add(place.to_y, own, full(0, place.z, y), 2)]
            self.far = along_z(0, other, full(0, place.z, other))
        if order == Z_Y_X and single:
            self.first = [same(place.to_y, 0, y, 0)]
        if order == Z_Y_X and not single:
            self.first = [links.add(place.to_y, own, full(0, place.z, y), 2)]
            for k in range(1, 4):
                block = full(0, place.zs[k], y)
                self.first.append(links.add(place.to_y, block, block, 2))
        self.second = [
            same(place.to_y, k, yy, k) if order == X_Z_Y else same(place.to_x, k, yy, 2)
            for k, yy in blocks[: 2 if last else 1]
        ]
        if not last:
            blocks = [block for block in blocks if block[0] == 0]
        self.core = [same(place.to_core, k, yy, k + 1) for k, yy in blocks]


Z_Y_X, Y_Z_X, X_Z_Y = range(3)


def fused_forward(
    tie_ref, len_ref, tokens_ref, gains_ref, bias_ref, in_ref, out_ref, expand_ref,
    project_ref,
    gq_ref, gw_ref, flat1_ref, flat2_ref, rows_ref,
    q_ref, v_ref, kt_ref, p_ref, scale_ref, o_ref, a1t_out, h1_out, a2_out, a2t_out,
    own0_ref, ownw_ref, own1_ref, own2_ref, square_ref, vec_ref,
    all0_ref, allw_ref, w1_ref, w2_ref, vecs_ref, bqv_ref, x_ref, a1_ref, k_ref, qa_ref, vt_ref, ot_ref, a1t_ref, h1_ref, a2_ref, a2t_ref,
    send_sem, recv_sem, local_sem, flush_sem, row_sem,
):
    t = pl.program_id(0)
    n, _ = x_ref.shape
    width = allw_ref.shape[-1]
    heads = width // HEAD_DIM
    step = 256
    place = Place()
    length = len_ref[place.t]
    links = Links(send_sem, recv_sem)
    z, y, x, c = place.z, place.y, place.x, place.c
    mine_there = vecs_ref.at[z, y, x, c]
    column = vecs_ref.at[:, :, x, c]
    vec_one = [links.add(device, vec_ref, mine_there) for device in place.same_t]
    vec_two = [links.add(device, column, column) for device in place.same_dp]
    seg0 = Gather(
        links, place, own0_ref, lambda k, z, y: all0_ref.at[k, z, y], Z_Y_X, single=False
    )
    segw = Gather(links, place, ownw_ref, lambda k, z, y: allw_ref.at[k, z, y], Z_Y_X)
    seg1 = Gather(
        links, place, own1_ref, lambda k, z, y: w1_ref.at[k, z, y], Y_Z_X, last=False
    )
    seg2 = Gather(
        links, place, own2_ref, lambda k, z, y: w2_ref.at[k, z, y], X_Z_Y, last=False
    )
    flush = [
        [
            pltpu.make_async_copy(ref.at[k], flat.at[k], flush_sem.at[i, k])
            for k in range(3)
        ]
        for i, (ref, flat) in enumerate([(w1_ref, flat1_ref), (w2_ref, flat2_ref)])
    ]
    put_a1t = pltpu.make_async_copy(a1t_ref, a1t_out, local_sem.at[0])
    put_a2t = pltpu.make_async_copy(a2t_ref, a2t_out, local_sem.at[1])
    puts = []
    for i in range(n // step):
        rows = pl.ds(i * step, step)
        puts.append([
            pltpu.make_async_copy(h1_ref.at[rows], h1_out.at[rows], row_sem.at[0, i]),
            pltpu.make_async_copy(a2_ref.at[rows], a2_out.at[rows], row_sem.at[1, i]),
        ])
    fetch = pltpu.make_async_copy(tokens_ref.at[place.t], x_ref, local_sem.at[2])

    def relay_z(copies):
        recv(copies[1])
        start(copies[2])

    def pass_own(seg):
        recv(seg.z[0], seg.z[2])
        weave(seg.first if seg is segw else [], seg.second[0], seg.core[0])

    def pass_second(seg):
        recv(seg.second)
        if seg is seg2:
            start(seg.core[1])

    def pass_first(seg):
        recv(seg.first)
        if seg is segw:
            weave(seg.second[1], seg.core[1])
        else:
            weave(seg.far[1], seg.far[0])

    def pass_far(seg):
        recv(seg.far[0], seg.far[2])
        start(seg.core[1:] if seg is seg1 else [])

    def pass_core(seg, i):
        recv(seg.second[i])
        start(seg.core[2 + i])

    plan = [
        (0, 0, lambda: (pass_own(segw), pass_first(seg1), relay_z(seg2.z), pass_first(seg2))),
        (0, 2, lambda: (pass_first(segw), relay_z(seg1.z), pass_core(seg0, 0))),
        (1, 0, lambda: recv(seg0.core[:2])),
        (1, 1, lambda: relay_z(seg1.far)),
        (1, 2, lambda: (
            pass_core(seg0, 1), recv(segw.core[:2]), pass_core(segw, 0), pass_own(seg2),
        )),
        (2, 1, lambda: relay_z(seg2.far)),
        (2, 2, lambda: (pass_core(segw, 1), pass_own(seg1))),
        (3, 0, lambda: (recv(seg0.core[2:]), pass_far(seg1), flush[0][0].start())),
        (3, 1, lambda: (pass_second(seg2), flush[1][0].start())),
        (3, 2, lambda: (pass_far(seg2), flush[1][2].start(), recv(segw.core[2:]))),
    ]

    def serve(point):
        for step, where, act in plan:
            if where == point:
                pl.when(t == step)(lambda act=act: (act(), None)[1])

    @pl.when(t == 0)
    def _():
        s0, s1, s2, s3 = tie_ref[0], tie_ref[1], tie_ref[2], tie_ref[3]
        fetch.start()
        square_ref[...] = jnp.zeros_like(square_ref)
        gain = gains_ref.shape[-1]
        square_ref[0:1, :gain] = gains_ref[s0].astype(F32)[0:1]
        square_ref[1:2, :gain] = gains_ref[s2].astype(F32)[1:2]
        kinds = [s0, s0, s0, s1, s2, s3, s2, s2, s2, s2]
        for i, source in enumerate(kinds):
            wide = bias_ref[i].astype(F32)
            here = lax.broadcasted_iota(jnp.int32, wide.shape, 0) == source
            square_ref[2 + i : 3 + i, :gain] = jnp.sum(
                jnp.where(here, wide, 0.0), 0, keepdims=True
            )
        vec_ref[...] = square_ref[...].T[:gain]
        for j in range(3):
            own0_ref[:, j * width : (j + 1) * width] = in_ref[s0, j]
        place.greet(place.same_t + place.same_dp)
        start(vec_one, seg0.z[1], seg0.z[0], seg0.first[0])
        vecs_ref[z, y, x, c] = vec_ref[...]
        ones = lax.broadcasted_iota(jnp.int32, (vt_ref.shape[1] - HEAD_DIM, n), 0) == 0
        for h in range(heads):
            vt_ref[h, HEAD_DIM:, :] = ones.astype(BF16)
        all0_ref[0, z, y] = own0_ref[...]
        ownw_ref[...] = out_ref[s1].T
        allw_ref[0, z, y] = ownw_ref[...]
        own1_ref[...] = expand_ref[s2]
        own2_ref[...] = project_ref[s3]
        w1_ref[0, z, y] = own1_ref[...]
        w2_ref[0, z, y] = own2_ref[...]
        recv(vec_one)
        start(vec_two)
        relay_z(seg0.z)
        start(seg0.first[2])
        recv(seg0.z[0])
        start(seg0.first[1], segw.z[1], segw.z[0], seg2.z[1])
        recv(vec_two)
        start(seg2.first)
        vecs = vecs_ref[...].reshape(D, vecs_ref.shape[-1]).T[:16]
        rows_ref[...] = vecs
        recv(seg0.z[2])
        start(seg0.first[3], seg1.first, seg2.z[0], seg1.z[1], seg1.z[0])
        weave(seg0.second[0], seg0.core[0])
        for k in range(4):
            part = slice(k * width, (k + 1) * width)
            bqv_ref[k, 0:1, :width] = vecs[3:4, part]
            bqv_ref[k, 0:1, width : 2 * width] = jnp.zeros((1, width), F32)
            bqv_ref[k, 0:1, 2 * width :] = vecs[4:5, part]
        fetch.wait()

        @pl.loop(0, n // step)
        def _(b):
            rows = pl.ds(pl.multiple_of(b * step, step), step)
            wide = x_ref[rows, :].astype(F32)
            xhat, _ = norm_parts(wide)
            a1 = (xhat * rows_ref[0:1, :] + rows_ref[2:3, :]).astype(BF16)
            a1_ref[rows, :] = a1
            a1t_ref[:, rows] = a1.T
            h1_ref[rows, :] = wide + rows_ref[5:6, :]

        put_a1t.start()
        relay_z(segw.z)
        recv(seg0.first)
        weave(seg0.second[1], seg0.core[1])

    serve(0)
    gq = all0_ref[t].reshape(D, 3 * width)
    gq_ref[0] = gq
    mine = place.group(t)
    qkv = dot_nn(a1_ref[...], gq) + bqv_ref[mine, 0:1, :]
    q = qkv[:, :width].astype(BF16) * jnp.asarray(HEAD_DIM ** -0.5, BF16)
    k = qkv[:, width : 2 * width].astype(BF16)
    v = qkv[:, 2 * width :].astype(BF16)
    q_ref[0] = q
    kt_ref[0] = k.T
    v_ref[0] = v
    vt = v.T
    for h in range(heads):
        vt_ref[h, :HEAD_DIM, :] = vt[h * HEAD_DIM : (h + 1) * HEAD_DIM]
    spare = k_ref.shape[1] - width
    dead = lax.broadcasted_iota(jnp.int32, (n, spare), 0) >= length
    first_column = lax.broadcasted_iota(jnp.int32, (n, spare), 1) == 0
    k_ref[:, :width] = k
    k_ref[:, width:] = jnp.where(first_column & dead, MASKED, 0.0).astype(BF16)
    qa_ref[:, :width] = q
    qa_ref[:, width:] = jnp.where(first_column, 1.0, 0.0).astype(BF16)

    serve(1)
    def scores(h, b):
        first, last = b * step, (b + 1) * step
        q = qa_ref[first:last, :]
        lane = lax.broadcasted_iota(jnp.int32, (1, q.shape[1]), 1)
        keep = head_mask((1, q.shape[1]), h) | (lane >= width)
        return dot_nt(k_ref[:last, :], jnp.where(keep, q, jnp.zeros((), BF16)))

    def attend(h, b, s):
        first, last = b * step, (b + 1) * step
        key = lax.broadcasted_iota(jnp.int32, (step, step), 0)
        query = lax.broadcasted_iota(jnp.int32, (step, step), 1)
        near = jnp.where(key <= query, s[first:], MASKED)
        top = jnp.max(near, 0, keepdims=True)
        if b:
            far = s[:first]
            top = jnp.maximum(top, jnp.max(far, 0, keepdims=True))
        e_near = jnp.exp((near - top).astype(BF16))
        p_ref[0, h, b, first:last, :] = e_near
        o = dot_nn(vt_ref[h, :, first:last], e_near)
        if b:
            e_far = jnp.exp((far - top).astype(BF16))
            p_ref[0, h, b, :first, :] = e_far
            o += dot_nn(vt_ref[h, :, :first], e_far)
        scale = 1.0 / o[HEAD_DIM : HEAD_DIM + 1]
        scale_ref[0, h : h + 1, first:last] = scale
        ot_ref[h * HEAD_DIM : (h + 1) * HEAD_DIM, first:last] = (
            o[:HEAD_DIM] * scale
        ).astype(BF16)

    scale_ref[0, heads:, :] = jnp.zeros((scale_ref.shape[1] - heads, n), F32)
    ready = [scores(h, 0) for h in range(heads)]
    for b in range(n // step):
        ahead = [scores(h, b + 1) for h in range(heads)] if b + 1 < n // step else None
        for h in range(heads):
            attend(h, b, ready[h])
        ready = ahead
    serve(2)

    gw_ref[0] = allw_ref[t].reshape(gw_ref.shape[1:])
    o = ot_ref[...].T
    o_ref[0] = o
    h1_ref[...] += dot_nt(o, gw_ref[0])

    @pl.when(t == 3)
    def _():
        for i, rows in enumerate(blocks(n, step)):
            xhat, _ = norm_parts(h1_ref[rows, :])
            a2 = (xhat * rows_ref[1:2, :] + rows_ref[6:7, :]).astype(BF16)
            a2_ref[rows, :] = a2
            a2t_ref[:, rows] = a2.T
            for put in puts[i]:
                put.start()
        put_a2t.start()
        recv(seg2.core)
        flush[1][1].start()
        recv(seg1.core)
        flush[0][1].start()
        pass_second(seg1)
        flush[0][2].start()
        links.sent()
        for copies in flush + puts + [[put_a1t, put_a2t]]:
            for copy in copies:
                copy.wait()


N_GATHER = 10 + 13 + 10 + 10 + 10
VMEM_WHOLE = pl.BlockSpec(memory_space=pltpu.VMEM)
ANY_WHOLE = pl.BlockSpec(memory_space=pl.ANY)


def run_fused_forward(tie, lengths, tokens, gains, biases, w_in, w_out, w_expand, w_project):
    groups, n, _ = tokens.shape
    depth, width = w_in.shape[-2:]
    heads = width // HEAD_DIM
    hidden = w_expand.shape[-1]
    w_project = w_project.transpose(0, 2, 1)
    biases = biases.transpose(1, 0, 2)
    own = gains.shape[-1]
    return pl.pallas_call(
        fused_forward,
        grid=(groups,),
        in_specs=[SMEM_WHOLE, SMEM_WHOLE, ANY_WHOLE] + [VMEM_WHOLE] * 6,
        out_specs=[
            group(D, 3 * width), group(D, width), ANY_WHOLE, ANY_WHOLE, VMEM_WHOLE,
            group(n, width), group(n, width), group(width, n), group(heads, n // 256, n, 256),
            group(8, n), group(n, width), ANY_WHOLE, ANY_WHOLE, ANY_WHOLE, ANY_WHOLE,
        ],
        out_shape=[
            shaped(BF16, groups, D, 3 * width), shaped(BF16, groups, D, width),
            shaped(BF16, groups, Z_DEV, Y_DEV, depth, hidden),
            shaped(BF16, groups, Z_DEV, Y_DEV, depth, hidden),
            shaped(F32, 16, D),
            shaped(BF16, groups, n, width), shaped(BF16, groups, n, width),
            shaped(BF16, groups, width, n), shaped(BF16, groups, heads, n // 256, n, 256),
            shaped(F32, groups, 8, n), shaped(BF16, groups, n, width), shaped(BF16, D, n), shaped(F32, n, D),
            shaped(BF16, n, D), shaped(BF16, D, n),
        ],
        scratch_shapes=[
            pltpu.VMEM((depth, 3 * width), BF16), pltpu.VMEM((depth, width), BF16),
            pltpu.VMEM((depth, hidden), BF16), pltpu.VMEM((depth, hidden), BF16),
            pltpu.VMEM((128, 128), F32), pltpu.VMEM((own, 128), F32),
            pltpu.VMEM((groups, Z_DEV, Y_DEV, depth, 3 * width), BF16),
            pltpu.VMEM((groups, Z_DEV, Y_DEV, depth, width), BF16),
            pltpu.VMEM((groups, Z_DEV, Y_DEV, depth, hidden), BF16),
            pltpu.VMEM((groups, Z_DEV, Y_DEV, depth, hidden), BF16),
            pltpu.VMEM((Z_DEV, Y_DEV, X_DEV, C_DEV, own, 128), F32),
            pltpu.VMEM((groups, 8, 3 * width), F32),
            pltpu.VMEM((n, D), BF16), pltpu.VMEM((n, D), BF16), pltpu.VMEM((n, 256), BF16),
            pltpu.VMEM((n, 256), BF16), pltpu.VMEM((heads, HEAD_DIM + 16, n), BF16),
            pltpu.VMEM((width, n), BF16),
            pltpu.VMEM((D, n), BF16), pltpu.VMEM((n, D), F32), pltpu.VMEM((n, D), BF16),
            pltpu.VMEM((D, n), BF16),
            pltpu.SemaphoreType.DMA((N_GATHER,)), pltpu.SemaphoreType.DMA((N_GATHER,)),
            pltpu.SemaphoreType.DMA((3,)), pltpu.SemaphoreType.DMA((2, 4)),
            pltpu.SemaphoreType.DMA((2, n // 256)),
        ],
        compiler_params=pltpu.CompilerParams(
            vmem_limit_bytes=VMEM_LIMIT, collective_id=0, has_side_effects=True
        ),
        name="fused_forward",
    )(tie, lengths, tokens, gains, biases, w_in, w_out, w_expand, w_project)


class Result:
    def __init__(self, links, place, own_ref, passing_ref, out_ref, step, sem, count):
        self.x, self.core, self.far, self.keep, self.keep_far = [], [], [], [], []
        for i in range(count):
            rows = pl.ds(i * step, step)
            mine, theirs = out_ref.at[place.t, rows], out_ref.at[place.ts[2], rows]
            own, passing = own_ref.at[rows], passing_ref.at[rows]
            self.x.append(links.add(place.to_x, own, passing))
            self.core.append(links.add(place.to_core, own, mine))
            self.far.append(links.add(place.to_core, passing, theirs))
            self.keep.append(pltpu.make_async_copy(own, mine, sem.at[0, i]))
            self.keep_far.append(pltpu.make_async_copy(passing, theirs, sem.at[1, i]))

    def send(self, i):
        start(self.x[i], self.core[i], self.keep[i])

    def pass_on(self, i):
        recv(self.x[i])
        start(self.far[i], self.keep_far[i])

    def finish(self):
        recv(self.core, self.far)
        for copy in self.keep + self.keep_far:
            copy.wait()


def low(value):
    return jnp.asarray(value, BF16)


def pair_order(i):
    return i + 1 - 2 * (i % 2)


def fused_feed_forward(
    len_ref, cot_ref, a2_ref, a2t_in, h1_in, far1_ref, far2_ref, rows_ref,
    out_out, fold_ref, work_out, dh1_out, gb_out, gbt_out, sums_ref,
    gf_ref, gft_ref, feed_ref, da2_ref, h_ref, df_ref, weights_ref, missing_ref, third_ref,
    stage_ref, land_ref, near_ref, cross_ref, a2t_ref, h1_ref, out_ref, work_ref,
    send_sem, recv_sem, local_sem, row_sem,
):
    t = pl.program_id(0)
    n = gf_ref.shape[0]
    step = 256
    depth = stage_ref.shape[-2]
    place = Place()
    length = len_ref[place.t]
    links = Links(send_sem, recv_sem)
    y, other = place.y, place.other_y
    last = [
        links.add(place.to_x, far1_ref.at[0, :, other], missing_ref.at[0, 0], Z_DEV),
        links.add(place.to_y, far2_ref.at[2, :, y], missing_ref.at[1, 0], Z_DEV),
    ]
    last_core = [
        links.add(place.to_core, missing_ref.at[i, 0], missing_ref.at[i, 1], Z_DEV)
        for i in range(2)
    ]
    third = [
        links.add(place.to_core, far_ref.at[2, :, y], third_ref.at[i], Z_DEV)
        for i, far_ref in enumerate([far1_ref, far2_ref])
    ]
    core = [
        [
            links.add(place.to_core, stage_ref.at[i], land_ref.at[s, i], Z_DEV) for i in range(2)
        ]
        for s in range(2)
    ]
    cross = [
        links.add(place.to_y, near_ref.at[i, :, other], cross_ref.at[i], Z_DEV)
        for i in range(2)
    ]
    fetch = pltpu.make_async_copy(cot_ref.at[place.t], gf_ref, local_sem.at[0])
    gb_ref, gbt_ref, dh1_ref = gf_ref, gft_ref, da2_ref
    late = [
        pltpu.make_async_copy(a2t_in, a2t_ref, local_sem.at[5]),
        pltpu.make_async_copy(h1_in, h1_ref, local_sem.at[6]),
    ]
    puts = []
    for i in range(n // step):
        rows = pl.ds(i * step, step)
        puts.append([
            pltpu.make_async_copy(ref.at[rows], out.at[rows], row_sem.at[j, i])
            for j, (ref, out) in enumerate(
                [(out_ref, out_out), (dh1_ref, dh1_out), (gb_ref, gb_out)]
            )
        ])
    put_gbt = pltpu.make_async_copy(gbt_ref, gbt_out, local_sem.at[7])
    put_work = pltpu.make_async_copy(work_ref, work_out, local_sem.at[8])
    k = pair_order(t)
    mine = place.group(k)

    def load(step, whole, slot):
        for i, far_ref in enumerate([far1_ref, far2_ref]):
            group = far_ref.at[pair_order(step)]
            to = weights_ref.at[slot, i]
            if not whole:
                group, to = group.at[:, y], to.at[:, y]
            yield pltpu.make_async_copy(group, to, local_sem.at[1 + 2 * slot + i])

    def live_rows(b):
        at = b * step + lax.broadcasted_iota(jnp.int32, (step, 1), 0)
        return (at < length).astype(F32)

    @pl.when(t == 0)
    def _():
        fetch.start()
        for copy in load(0, True, 0):
            copy.start()
        for copy in late:
            copy.start()
        place.greet()
        weave(last, third)
        sums_ref[...] = jnp.zeros_like(sums_ref)
        feed_ref[...] = jnp.zeros_like(feed_ref)
        da2_ref[...] = jnp.zeros_like(da2_ref)
        fetch.wait()

        @pl.loop(0, n // step)
        def _(b):
            rows = pl.ds(pl.multiple_of(b * step, step), step)
            g = (gf_ref[rows, :].astype(F32) * live_rows(b)).astype(BF16)
            gf_ref[rows, :] = g
            gft_ref[:, rows] = g.T
            sums_ref[7:8, :] += jnp.sum(g.astype(F32), 0, keepdims=True)

    for i in range(4):
        @pl.when(t == i)
        def _():
            if i == 2:
                recv(last_core, third)
            else:
                for copy in load(i, i < 2, i % 2):
                    copy.wait()
            if i in (0, 2):
                for copy in load(i + 1, i + 1 < 2, (i + 1) % 2):
                    copy.start()
            for j in range(2):
                if i == 2:
                    weights_ref[0, j, :, y] = third_ref[j]
                if i >= 2:
                    weights_ref[i % 2, j, :, other] = missing_ref[j, 3 - i]

    bias = rows_ref[pl.ds(8 + mine, 1), :]
    w1 = weights_ref[t % 2, 0].reshape(D, -1)
    w2 = weights_ref[t % 2, 1].reshape(D, -1)
    column = jnp.zeros((1, w1.shape[1]), F32)
    for rows in blocks(n, step):
        f = (dot_nn(a2_ref[rows, :], w1) + bias).astype(BF16)
        dh = dot_nn(gf_ref[rows, :], w2)
        f2 = f * f
        th = jnp.tanh(f * (low(SQRT_2_PI) + low(SQRT_2_PI * 0.044715) * f2))
        half = low(0.5) + low(0.5) * th
        h = f * half
        slope = half + f * (low(0.5) - low(0.5) * th * th) * (
            low(SQRT_2_PI) + low(3 * SQRT_2_PI * 0.044715) * f2
        )
        df = (dh * slope.astype(F32)).astype(BF16)
        h_ref[rows, :] = h
        df_ref[rows, :] = df
        column += jnp.sum(df.astype(F32), 0, keepdims=True)
        feed_ref[rows, :] += dot_nt(h, w2)
        da2_ref[rows, :] += dot_nt(df, w1)
    sums_ref[pl.ds(8 + mine, 1), :] = column

    @pl.when(t == 1)
    def _():
        recv(last)
        start(last_core)

    @pl.when(t == 0)
    def _():
        late[0].wait()

    def weight_grad(left_ref, right_ref):
        value = dot_nn(left_ref[...], right_ref[...])
        return value.reshape(Z_DEV, Y_DEV, depth, value.shape[-1]).astype(BF16)

    grad1 = weight_grad(a2t_ref, df_ref)
    grad2 = weight_grad(gft_ref, h_ref)

    def put(ref):
        ref[0] = grad1
        ref[1] = grad2

    def reduced(ref):
        return lambda i, s, z: (
            ref[i, z].astype(F32) + land_ref[s, i, z].astype(F32)
        ).astype(BF16)

    @pl.when(t == 0)
    def _():
        put(stage_ref)
        start(core[0])

    @pl.when(t == 1)
    def _():
        put(near_ref)
        recv(core[0])

        @pl.loop(0, Z_DEV)
        def _(z):
            for i in range(2):
                near_ref[i, z] = reduced(near_ref)(i, 0, z)

        weave(cross)

    @pl.when(t == 2)
    def _():
        for copy in core[0]:
            copy.wait_send()
        put(stage_ref)
        start(core[1])

    @pl.when(t == 3)
    def _():
        put(work_ref)
        late[1].wait()
        for i, rows in enumerate(blocks(n, step)):
            live = live_rows(i)
            h1 = h1_ref[rows, :]
            out_ref[rows, :] = (live * (h1 + (feed_ref[rows, :] + rows_ref[7:8, :]))).astype(BF16)
            xhat, r = norm_parts(h1)
            da2 = da2_ref[rows, :]
            sums_ref[1:2, :] += jnp.sum(da2 * xhat, 0, keepdims=True)
            sums_ref[6:7, :] += jnp.sum(da2, 0, keepdims=True)
            dg = da2 * rows_ref[1:2, :]
            dv = r * (
                dg
                - jnp.mean(dg, -1, keepdims=True)
                - xhat * jnp.mean(dg * xhat, -1, keepdims=True)
            )
            dh1 = gf_ref[rows, :].astype(F32) + dv
            dh1_ref[rows, :] = dh1
            gb = dh1.astype(BF16)
            gb_ref[rows, :] = gb
            gbt_ref[:, rows] = gb.T
            sums_ref[5:6, :] += jnp.sum(gb.astype(F32), 0, keepdims=True)
            for copy in puts[i]:
                copy.start()
        put_gbt.start()
        recv(core[1])

        @pl.loop(0, Z_DEV)
        def _(z):
            for i in range(2):
                work_ref[i, z] = reduced(work_ref)(i, 1, z)

        put_work.start()
        recv(cross)

        @pl.loop(0, Z_DEV)
        def _(z):
            for i in range(2):
                fold_ref[i, z] = (
                    near_ref[i, z, y].astype(F32) + cross_ref[i, z].astype(F32)
                ).astype(BF16)

        links.sent(*core[0])
        for copies in puts + [[put_gbt, put_work]]:
            for copy in copies:
                copy.wait()


def run_fused_feed_forward(lengths, cot, a2, a2t, h1, g1, g2, rows):
    n = cot.shape[1]
    groups, _, _, depth, hidden = g1.shape
    both = (2, Z_DEV, Y_DEV, depth, hidden)
    fold = (2, Z_DEV, depth, hidden)
    return pl.pallas_call(
        fused_feed_forward,
        grid=(groups,),
        in_specs=[SMEM_WHOLE, ANY_WHOLE, VMEM_WHOLE] + [ANY_WHOLE] * 4 + [VMEM_WHOLE],
        out_specs=[ANY_WHOLE, VMEM_WHOLE] + [ANY_WHOLE] * 4 + [VMEM_WHOLE],
        out_shape=[
            shaped(BF16, n, D), shaped(BF16, *fold), shaped(BF16, *both), shaped(F32, n, D),
            shaped(BF16, n, D), shaped(BF16, D, n), shaped(F32, 16, D),
        ],
        scratch_shapes=[
            pltpu.VMEM((n, D), BF16), pltpu.VMEM((D, n), BF16), pltpu.VMEM((n, D), F32),
            pltpu.VMEM((n, D), F32), pltpu.VMEM((n, hidden), BF16), pltpu.VMEM((n, hidden), BF16),
            pltpu.VMEM((2,) + both, BF16),
            pltpu.VMEM((2,) + fold, BF16), pltpu.VMEM(fold, BF16), pltpu.VMEM(both, BF16),
            pltpu.VMEM((2,) + both, BF16),
            pltpu.VMEM(both, BF16), pltpu.VMEM(fold, BF16),
            pltpu.VMEM((D, n), BF16), pltpu.VMEM((n, D), F32), pltpu.VMEM((n, D), BF16),
            pltpu.VMEM(both, BF16),
            pltpu.SemaphoreType.DMA((12,)), pltpu.SemaphoreType.DMA((12,)),
            pltpu.SemaphoreType.DMA((9,)), pltpu.SemaphoreType.DMA((3, n // 256)),
        ],
        compiler_params=pltpu.CompilerParams(
            vmem_limit_bytes=VMEM_LIMIT, collective_id=1, has_side_effects=True
        ),
        name="fused_feed_forward",
    )(lengths, cot, a2, a2t, h1, g1, g2, rows)
class Reduce:
    def __init__(
        self, links, place, work, acc, cross_ref, far_ref, mid_ref, last_ref, side_ref,
        slots=(0, 1),
    ):
        self.place, self.work, self.acc = place, work, acc
        self.cross_ref, self.far_ref, self.mid_ref = cross_ref, far_ref, mid_ref
        self.last_ref, self.side_ref = last_ref, side_ref
        zs = place.zs
        self.y = {
            s: [
                links.add(
                    place.to_y, work(s, zs[j], place.other_y), cross_ref.at[s, zs[j]], 2
                )
                for j in (1, 3, 2, 0)
            ]
            for s in slots
        }
        self.z = [
            [
                links.add(place.to_z[1], acc(s, zs[1]), far_ref.at[s, 0], 2),
                links.add(place.to_z[1], acc(s, zs[3]), far_ref.at[s, 1], 2),
                links.add(place.to_z[2], mid_ref.at[s, 1], far_ref.at[s, 2], 2),
            ]
            for s in range(2)
        ]
        self.x = links.add(place.to_x, last_ref, side_ref, 2)

    def fold_y(self, s, half):
        for i, j in [(0, 1), (1, 3), (2, 2), (3, 0)][2 * half : 2 * half + 2]:
            z = self.place.zs[j]
            recv(self.y[s][i])
            value = self.work(s, z, self.place.y)[...].astype(F32)
            self.acc(s, z)[...] = (value + self.cross_ref[s, z].astype(F32)).astype(BF16)
            if i < 2:
                start(self.z[s][i])

    def fold_z(self, s):
        recv(self.z[s][:2])
        for i in (1, 0):
            value = self.acc(s, self.place.zs[2 * i])[...].astype(F32)
            self.mid_ref[s, i] = (value + self.far_ref[s, i].astype(F32)).astype(BF16)
            if i:
                start(self.z[s][2])

    def own(self, s):
        recv(self.z[s][2])
        return self.mid_ref[s, 0].astype(F32) + self.far_ref[s, 2].astype(F32)

    def send_x(self):
        self.last_ref[...] = self.own(1).astype(BF16)
        start(self.x)

    def total(self):
        value = self.own(0)
        recv(self.x)
        return value + self.side_ref[...].astype(F32)


def fused_backward(
    tokens_ref, gq_in, gw_in, rows_ref, dh1_ref, gb_ref, gbt_in, q_in, v_in, kt_in,
    p_ref, scale_in, o_in, a1t_in, layer_in, fold_in, work_in, early_ref,
    out_ref, layerout_ref, part0_ref, partw_ref, part1_ref, part2_ref, total_ref,
    gq_ref, gw_ref, q_ref, v_ref, kt_ref, scale_ref, o_ref,
    a1t_ref, gbt_ref, layer_ref, fold_ref, work_ref, do_ref, delta_ref, dkv_ref, dqkv_ref, da1_ref, own_ref, passing_ref, passlayer_ref, bqv_ref,
    folded_ref, cross1_ref, far1_ref, mid1_ref, last1_ref, side1_ref,
    cross2_ref, far2_ref, mid2_ref, last2_ref, side2_ref,
    stagew_ref, landw_ref, workw_ref, crossw_ref, farw_ref, midw_ref, lastw_ref, sidew_ref,
    stage0_ref, land0_ref, work0_ref, cross0_ref, far0_ref, mid0_ref, last0_ref, side0_ref,
    sums_ref, sumland_ref,
    send_sem, recv_sem, local_sem, result_sem, group_sem,
):
    t = pl.program_id(0)
    n = own_ref.shape[0]
    width = gw_ref.shape[-1]
    depth = part0_ref.shape[0]
    heads = width // HEAD_DIM
    step = n // 4
    place = Place()
    y = place.y
    links = Links(send_sem, recv_sem)
    k, i = group_and_block(t)
    mine = place.group(k)
    now = k % 2
    out = Result(links, place, own_ref, passing_ref, out_ref, step // 2, result_sem.at[0], 8)
    layer = Result(links, place, layer_ref, passlayer_ref, layerout_ref, step // 2, result_sem.at[1], 8)
    fetch = pltpu.make_async_copy(tokens_ref.at[place.t], own_ref, local_sem.at[0])
    fetch_layer, fetch_work, fetch_fold, fetch_gbt, fetch_a1t = [
        pltpu.make_async_copy(there, here, local_sem.at[1 + j])
        for j, (there, here) in enumerate([
            (layer_in, layer_ref), (work_in, work_ref), (fold_in, fold_ref),
            (gbt_in, gbt_ref), (a1t_in, a1t_ref),
        ])
    ]
    def operands(group):
        slot = group % 2
        pairs = [
            (gw_in, gw_ref), (scale_in, scale_ref), (o_in, o_ref), (v_in, v_ref),
            (q_in, q_ref), (kt_in, kt_ref), (gq_in, gq_ref),
        ]
        return [
            pltpu.make_async_copy(there.at[group], here.at[slot], group_sem.at[slot, j])
            for j, (there, here) in enumerate(pairs)
        ]

    corew = [links.add(place.to_core, stagew_ref, landw_ref.at[i], Z_DEV) for i in range(2)]
    core0 = [links.add(place.to_core, stage0_ref, land0_ref.at[i], Z_DEV) for i in range(2)]
    def half_done(i, *landing):
        return Reduce(
            links, place, lambda s, z, y: work_ref.at[i, z, y],
            lambda s, z: folded_ref.at[i, z] if s else fold_ref.at[i, z],
            *landing, slots=(1,),
        )

    seg1 = half_done(0, cross1_ref, far1_ref, mid1_ref, last1_ref, side1_ref)
    seg2 = half_done(1, cross2_ref, far2_ref, mid2_ref, last2_ref, side2_ref)
    segw = Reduce(
        links, place, lambda s, z, y: workw_ref.at[s, z, y],
        lambda s, z: workw_ref.at[s, z, y],
        crossw_ref, farw_ref, midw_ref, lastw_ref, sidew_ref,
    )
    seg0 = Reduce(
        links, place, lambda s, z, y: work0_ref.at[s, z, y],
        lambda s, z: work0_ref.at[s, z, y],
        cross0_ref, far0_ref, mid0_ref, last0_ref, side0_ref,
    )
    sum_core, sum_y, *sum_z, sum_x = [
        links.add(to, sums_ref.at[i], sumland_ref.at[j])
        for j, (i, to) in enumerate(
            zip([0, 1, 2, 2, 2, 3], [place.to_core, place.to_y] + place.to_z[1:] + [place.to_x])
        )
    ]

    def when(point):
        return pl.when(t == point)

    @when(0)
    def _():
        start(fetch_layer, operands(1), fetch_work, fetch_fold, fetch_gbt, operands(0))
        start(fetch, fetch_a1t)
        place.greet()
        for copy in (fetch_layer, fetch_work, fetch_fold):
            copy.wait()
        across = [*seg1.y[1], *seg2.y[1]]
        along = [*seg1.z[0][:2], *seg2.z[0][:2]]
        for i in range(8):
            start(across[i], along[i // 2] if i % 2 == 0 else [])
            layer.send(i)
        bqv_ref[...] = jnp.zeros_like(bqv_ref)
        sums_ref[0] = early_ref[...]
        fetch_gbt.wait()

    def add_core():
        recv(corew[1])

        @pl.loop(0, Z_DEV)
        def _(z):
            workw_ref[1, z] = (
                workw_ref[1, z].astype(F32) + landw_ref[1, z].astype(F32)
            ).astype(BF16)

        start(segw.y[1])

    def wait(copies):
        for copy in copies:
            copy.wait()

    @when(0)
    def _():
        wait(operands(1))

    @when(4)
    def _():
        start(operands(3))
        wait(operands(0))

    @when(8)
    def _():
        start(operands(2))
        wait(operands(3))

    @when(9)
    def _():
        wait(operands(2))

    plan = [
        (2, 1, lambda: (seg1.fold_y(1, 0), seg1.fold_z(0))),
        (3, 1, lambda: (layer.pass_on(0), layer.pass_on(1))),
        (4, 0, lambda: (seg1.fold_y(1, 1), seg2.fold_z(0))),
        (5, 0, lambda: (layer.pass_on(2), layer.pass_on(3))),
        (5, 1, lambda: (seg1.fold_z(1), seg2.fold_y(1, 0))),
        (8, 0, lambda: (seg2.fold_y(1, 1), layer.pass_on(4), layer.pass_on(5))),
        (8, 1, lambda: (seg1.send_x(), segw.fold_y(0, 0), segw.fold_y(0, 1))),
        (9, 0, add_core),
        (9, 1, lambda: (seg2.fold_z(1), seg0.fold_y(0, 0), layer.pass_on(6), layer.pass_on(7))),
        (10, 1, lambda: segw.fold_z(0)),
        (11, 1, lambda: (seg2.send_x(), seg0.fold_y(0, 1))),
        (12, 1, lambda: (segw.fold_y(1, 0), segw.fold_y(1, 1))),
        (13, 1, lambda: (seg0.fold_z(0), out.pass_on(7), out.pass_on(6))),
        (14, 1, lambda: segw.fold_z(1)),
    ]

    def serve(point):
        for at, where, act in plan:
            if where == point:
                pl.when(t == at)(lambda act=act: (act(), None)[1])

    @pl.when((t == 0) | (t == 4) | (t == 8) | (t == 9))
    def _():
        pick = (
            lax.broadcasted_iota(jnp.int32, (8, width), 1) // HEAD_DIM
            == lax.broadcasted_iota(jnp.int32, (8, width), 0)
        ).astype(BF16)

        @pl.loop(0, n // step)
        def _(i):
            rows = pl.ds(pl.multiple_of(i * step, step), step)
            columns = scale_ref[now, :, rows].T
            lane = lax.broadcasted_iota(jnp.int32, (step, width), 1)
            scale = columns[:, heads - 1 : heads]
            for h in reversed(range(heads - 1)):
                scale = jnp.where(lane < (h + 1) * HEAD_DIM, columns[:, h : h + 1], scale)
            do = (dot_nn(gb_ref[rows, :], gw_ref[now]) * scale).astype(BF16)
            do_ref[now, rows, :] = do
            product = do.astype(F32) * o_ref[now, rows, :].astype(F32)
            high = product.astype(BF16)
            low = (product - high.astype(F32)).astype(BF16)
            delta_ref[now, :, rows] = dot_nt(pick, high) + dot_nt(pick, low)

        value = dot_nn(gbt_ref[...], o_ref[now]).reshape(Z_DEV, Y_DEV, depth, width)
        for s in range(2):
            @when(8 * s)
            def _():
                if s:
                    corew[0].wait_send()
                stagew_ref[...] = value.astype(BF16)
                start(corew[s])

        @when(4)
        def _():
            recv(corew[0])
            workw_ref[0] = (value + landw_ref[0].astype(F32)).astype(BF16)
            start(segw.y[0])

        @when(9)
        def _():
            workw_ref[1] = value.astype(BF16)

    serve(0)

    for ii in reversed(range(4)):
        @pl.when(i == ii)
        def _():
            first, last = ii * step, (ii + 1) * step
            do = do_ref[now, first:last, :]
            q = q_ref[now, first:last, :]
            v = v_ref[now, :last, :]
            lane = lax.broadcasted_iota(jnp.int32, (1, width), 1)
            dk, dv, dq = None, None, []
            for h in range(heads):
                low, high = h * HEAD_DIM, (h + 1) * HEAD_DIM
                here = (lane >= low) & (lane < high)
                p = p_ref[0, h, 0, :last, :]
                dp = dot_nt(v, jnp.where(here, do, jnp.zeros((), BF16)))
                ds = p * (dp - delta_ref[now, h : h + 1, first:last]).astype(BF16)
                part = dot_nn(p, do)
                dv = part if dv is None else jnp.where(lane < low, dv, part)
                part = dot_nn(ds, q)
                dk = part if dk is None else jnp.where(lane < low, dk, part)
                dq.append(dot_nn(kt_ref[now, low:high, :last], ds))
            if ii == 3:
                dkv_ref[now, 0] = dk
                dkv_ref[now, 1] = dv
            else:
                dkv_ref[now, 0, :last, :] += dk
                dkv_ref[now, 1, :last, :] += dv
            dk = dkv_ref[now, 0, first:last, :].astype(BF16)
            dv = dkv_ref[now, 1, first:last, :].astype(BF16)
            dq = (jnp.concatenate(dq, 0) * HEAD_DIM ** -0.5).astype(BF16).T
            dqkv_ref[now, first:last, :width] = dq
            dqkv_ref[now, first:last, width : 2 * width] = dk
            dqkv_ref[now, first:last, 2 * width :] = dv
            bqv_ref[mine, 0:1, :] += jnp.sum(dq.astype(F32), 0, keepdims=True)
            bqv_ref[mine, 1:2, :] += jnp.sum(dv.astype(F32), 0, keepdims=True)

            @pl.when(t >= 8)
            def _():
                da1_ref[first:last, :] += dot_nt(dqkv_ref[now, first:last, :], gq_ref[now])

    serve(1)

    @pl.when((t > 8) & (t % 2 == 1))
    def _():
        rows = pl.ds(pl.multiple_of(i * step, step), step)
        xhat, r = norm_parts(own_ref[rows, :].astype(F32))
        da1 = da1_ref[rows, :]
        sums_ref[0, 0:1, :] += jnp.sum(da1 * xhat, 0, keepdims=True)
        sums_ref[0, 2:3, :] += jnp.sum(da1, 0, keepdims=True)
        dg = da1 * rows_ref[0:1, :]
        dv = r * (
            dg
            - jnp.mean(dg, -1, keepdims=True)
            - xhat * jnp.mean(dg * xhat, -1, keepdims=True)
        )
        own_ref[rows, :] = (dh1_ref[...] + dv).astype(BF16)
        for ii in range(4):
            @pl.when(i == ii)
            def _():
                out.send(2 * ii + 1)
                out.send(2 * ii)

    @pl.when((t == 3) | (t == 7) | (t > 13))
    def _():
        @when(3)
        def _():
            fetch.wait()
            fetch_a1t.wait()

        @when(3)
        def _():
            da1_ref[...] = dot_nt(dqkv_ref[now], gq_ref[now])

        @when(7)
        def _():
            da1_ref[...] += dot_nt(dqkv_ref[now], gq_ref[now])

        value = dot_nn(a1t_ref[...], dqkv_ref[now]).reshape(Z_DEV, Y_DEV, depth, 3 * width)
        for s in range(2):
            @when(3 + 11 * s)
            def _():
                if s:
                    core0[0].wait_send()
                stage0_ref[...] = value.astype(BF16)
                start(core0[s])

            @when(7 + 8 * s)
            def _():
                recv(core0[s])
                work0_ref[s] = (value + land0_ref[s].astype(F32)).astype(BF16)
                start(seg0.y[s])

    @when(15)
    def _():
        for s in range(4):
            sums_ref[0, 3:5, s * width : (s + 1) * width] = bqv_ref[s, 0:2, :]
        start(sum_core)
        segw.send_x()
        out.pass_on(5)
        out.pass_on(4)
        recv(sum_core)
        sums_ref[1] = sums_ref[0] + sumland_ref[0]
        start(sum_y)
        seg0.fold_y(1, 0)
        out.pass_on(3)
        out.pass_on(2)
        seg0.fold_y(1, 1)
        recv(sum_y)
        sums_ref[2] = sums_ref[1] + sumland_ref[1]
        start(sum_z)
        seg0.fold_z(1)
        recv(sum_z)
        sums_ref[3] = (sums_ref[2] + sumland_ref[2]) + (sumland_ref[3] + sumland_ref[4])
        start(sum_x)
        part1_ref[...] = seg1.total()
        part2_ref[...] = seg2.total()
        seg0.send_x()
        partw_ref[...] = segw.total()
        layer.finish()
        out.pass_on(1)
        out.pass_on(0)
        recv(sum_x)
        total_ref[...] = sums_ref[3] + sumland_ref[5]
        part0_ref[...] = seg0.total()
        out.finish()
        links.sent(corew[0], core0[0])


def group_and_block(t):
    early = t < 8
    return (
        jnp.where(early, 1 - t // 4, 3 - t % 2),
        3 - jnp.where(early, t % 4, jnp.maximum(t - 8, 0) // 2),
    )


def run_fused_backward(
    tokens, gq, gw, rows, dh1, gb, gbt, q, v, kt, p, scale, o, a1t, layer, fold, work, early
):
    groups, n, _ = tokens.shape
    width = gw.shape[-1]
    heads = width // HEAD_DIM
    hidden = fold.shape[-1]
    depth = D // (Z_DEV * Y_DEV)
    step = n // 4

    p_spec = pl.BlockSpec(
        (1, heads, 1, n, step),
        lambda t: (group_and_block(t)[0], 0, group_and_block(t)[1], 0, 0),
    )

    copies = 2 * 24 + 4 + 2 * 15 + 2 * 11 + 6

    def landing(lanes):
        return [
            pltpu.VMEM((2, Z_DEV, depth, lanes), BF16),
            pltpu.VMEM((2, 3, depth, lanes), BF16), pltpu.VMEM((2, 2, depth, lanes), BF16),
            pltpu.VMEM((depth, lanes), BF16), pltpu.VMEM((depth, lanes), BF16),
        ]

    def working(lanes):
        block = (Z_DEV, Y_DEV, depth, lanes)
        return [pltpu.VMEM(block, BF16)] + [pltpu.VMEM((2,) + block, BF16)] * 2

    return pl.pallas_call(
        fused_backward,
        grid=(4 * groups,),
        in_specs=[
            ANY_WHOLE, ANY_WHOLE, ANY_WHOLE, VMEM_WHOLE,
            pl.BlockSpec((step, D), lambda t: (group_and_block(jnp.maximum(t, 8))[1], 0)),
            VMEM_WHOLE, ANY_WHOLE, ANY_WHOLE, ANY_WHOLE, ANY_WHOLE, p_spec,
            ANY_WHOLE, ANY_WHOLE, ANY_WHOLE, ANY_WHOLE, ANY_WHOLE, ANY_WHOLE, VMEM_WHOLE,
        ],
        out_specs=[ANY_WHOLE] * 2 + [VMEM_WHOLE] * 5,
        out_shape=[
            shaped(BF16, groups, n, D), shaped(BF16, groups, n, D),
            shaped(F32, depth, 3 * width),
            shaped(F32, depth, width), shaped(F32, depth, hidden),
            shaped(F32, depth, hidden), shaped(F32, 16, D),
        ],
        scratch_shapes=[
            pltpu.VMEM((2, D, 3 * width), BF16), pltpu.VMEM((2, D, width), BF16),
            pltpu.VMEM((2, n, width), BF16), pltpu.VMEM((2, n, width), BF16),
            pltpu.VMEM((2, width, n), BF16), pltpu.VMEM((2, 8, n), F32),
            pltpu.VMEM((2, n, width), BF16),
            pltpu.VMEM((D, n), BF16), pltpu.VMEM((D, n), BF16), pltpu.VMEM((n, D), BF16),
            pltpu.VMEM((2, Z_DEV, depth, hidden), BF16),
            pltpu.VMEM((2, Z_DEV, Y_DEV, depth, hidden), BF16),
            pltpu.VMEM((2, n, width), BF16),
            pltpu.VMEM((2, 8, n), F32), pltpu.VMEM((2, 2, n, width), F32),
            pltpu.VMEM((2, n, 3 * width), BF16), pltpu.VMEM((n, D), F32),
            pltpu.VMEM((n, D), BF16), pltpu.VMEM((n, D), BF16), pltpu.VMEM((n, D), BF16),
            pltpu.VMEM((groups, 8, width), F32),
        ]
        + landing(hidden)[:1] + landing(hidden) + landing(hidden)
        + working(width) + landing(width)
        + working(3 * width) + landing(3 * width)
        + [
            pltpu.VMEM((4, 16, D), F32), pltpu.VMEM((6, 16, D), F32),
            pltpu.SemaphoreType.DMA((copies,)), pltpu.SemaphoreType.DMA((copies,)),
            pltpu.SemaphoreType.DMA((6,)), pltpu.SemaphoreType.DMA((2, 2, 8)),
            pltpu.SemaphoreType.DMA((2, 7)),
        ],
        compiler_params=pltpu.CompilerParams(
            vmem_limit_bytes=VMEM_LIMIT, collective_id=2, has_side_effects=True
        ),
        name="fused_backward",
    )(tokens, gq, gw, rows, dh1, gb, gbt, q, v, kt, p, scale, o, a1t, layer, fold, work, early)


def place_gradients(
    tie_ref, sums_ref, part0_ref, partw_ref, part1_ref, part2_ref, near_out_ref,
    near_grad_ref, far_out_ref, far_grad_ref, gains_ref, bias_ref, in_ref, out_ref, expand_ref,
    project_ref,
):
    far_out_ref[...] = near_out_ref[...]
    far_grad_ref[...] = near_grad_ref[...]
    own = gains_ref.shape[-1]
    width = partw_ref.shape[-1]

    @pl.when(pl.program_id(0) == 0)
    def _():
        first = (lax.axis_index("dp") * 4 + lax.axis_index("tensor")) * own
        feature = lax.broadcasted_iota(jnp.int32, (D, 128), 0)
        lane = lax.broadcasted_iota(jnp.int32, (D, 128), 1)
        chosen = ((feature == first + lane) & (lane < own)).astype(F32)
        sums = lax.dot_general(
            sums_ref[...], chosen, (((1,), (0,)), ((), ())),
            precision=lax.Precision.HIGHEST, preferred_element_type=F32,
        )[:, :own]
        s0, s1, s2, s3 = tie_ref[0], tie_ref[1], tie_ref[2], tie_ref[3]
        w_out = partw_ref[...].T

        def at(source, wanted, value):
            return jnp.where(source == wanted, value, jnp.zeros_like(value))

        row = lax.broadcasted_iota(jnp.int32, (NSRC, own), 0)
        for i, wanted in enumerate([s0, s0, s0, s1, s2, s3, s2, s2, s2, s2]):
            bias_ref[i] = jnp.where(row == wanted, sums[2 + i : 3 + i], 0.0)
        for s in range(NSRC):
            gains_ref[s, 0:1] = at(s, s0, sums[0:1])
            gains_ref[s, 1:2] = at(s, s2, sums[1:2])
            for j in range(3):
                in_ref[s, j] = at(s, s0, part0_ref[:, j * width : (j + 1) * width])
            out_ref[s] = at(s, s1, w_out)
            expand_ref[s] = at(s, s2, part1_ref[...])
            project_ref[s] = at(s, s3, part2_ref[...])


def run_place_gradients(tie, sums, part0, partw, part1, part2, out, grad, like):
    slots, n, _ = grad.shape
    gains, biases, w_in, w_out, w_expand, w_project = [item.shape for item in like]
    shapes = [
        gains, (biases[1], biases[0], biases[2]), w_in, w_out, w_expand,
        (w_project[0], w_project[2], w_project[1]),
    ]
    out, grad, gains, biases, w_in, w_out, w_expand, w_project = pl.pallas_call(
        place_gradients,
        grid=(slots,),
        in_specs=[SMEM_WHOLE] + [VMEM_WHOLE] * 5
        + [group(n, D), group(n, D)],
        out_specs=[group(n, D), group(n, D)] + [VMEM_WHOLE] * 6,
        out_shape=[shaped(BF16, slots, n, D)] * 2 + [shaped(F32, *item) for item in shapes],
        compiler_params=pltpu.CompilerParams(vmem_limit_bytes=VMEM_LIMIT),
        name="place_gradients",
    )(tie, sums, part0, partw, part1, part2, out, grad)
    biases = biases.transpose(1, 0, 2)
    return out, grad, gains, biases, w_in, w_out, w_expand, w_project.transpose(0, 2, 1)


def plain_step(
    tokens, lengths, tie_map, norm_gains, bias_rows, attention_in, attention_out,
    expand_weight, project_weight, cotangent,
):
    slot_rows = tokens.shape[0] // lengths.shape[0]
    me = lax.axis_index("tensor")
    in_local = lax.dynamic_index_in_dim(attention_in, tie_map[0], 0, keepdims=False)
    out_local = lax.dynamic_index_in_dim(attention_out, tie_map[1], 0, keepdims=False)
    expand_local = lax.dynamic_index_in_dim(expand_weight, tie_map[2], 0, keepdims=False)
    project_local = lax.dynamic_index_in_dim(project_weight, tie_map[3], 0, keepdims=False)
    local0 = jnp.concatenate([in_local, out_local.T[None]], 0)
    row_kinds = jnp.array([0, 0, 0, 1, 2, 3] + [2] * (FF // D), dtype=jnp.int32)
    gain_kinds = jnp.array([0, 2], dtype=jnp.int32)
    gain_pick = norm_gains[tie_map[gain_kinds], jnp.arange(2)]
    bias_pick = bias_rows[tie_map[row_kinds], jnp.arange(row_kinds.shape[0])]
    vectors = jnp.concatenate([gain_pick, bias_pick], 0)
    x = lax.dynamic_slice_in_dim(tokens, me * slot_rows, slot_rows, 0)
    cot = lax.dynamic_slice_in_dim(cotangent, me * slot_rows, slot_rows, 0)
    length = lax.dynamic_slice_in_dim(lengths, me, 1, 0)
    rows = lax.all_gather(vectors, ("dp", "tensor"), axis=1, tiled=True).astype(F32)
    rows = jnp.concatenate([rows, jnp.zeros((4, D), F32)], 0)

    def gathered(piece, axis):
        piece = lax.all_gather(piece, "dp", axis=axis, tiled=True)
        return lax.all_gather(piece, "tensor", axis=0)

    g0 = gathered(local0, 1)
    g1 = gathered(expand_local, 0)
    g2 = gathered(project_local.T, 0)
    groups, width = g0.shape[0], g0.shape[-1]
    bqv = rows[3:5].reshape(2, groups, width).transpose(1, 0, 2)
    q, v, kt, p, o, a1t, h1, a2, a2t = run_attention_forward(length, x, g0, rows, bqv)
    out, d1, d2, dh1, gb, gbt, sums = run_feed_forward(length, cot, a2, a2t, h1, g1, g2, rows)
    d0, xg, sums_in, sums_qv = run_attention_backward(
        x, g0, rows, dh1, gb, gbt, q, v, kt, p, o, a1t
    )
    layer_out = lax.all_gather(out, "tensor", axis=0, tiled=True)
    tokens_grad = lax.all_gather(xg, "tensor", axis=0, tiled=True)

    def scattered(piece, axis):
        piece = lax.psum_scatter(piece, "tensor", scatter_dimension=0)
        return lax.psum_scatter(piece, "dp", scatter_dimension=axis, tiled=True).astype(F32)

    part0 = scattered(d0, 1)
    part1 = scattered(d1, 0)
    part2 = scattered(d2, 0)
    qv = sums_qv[:, :2].transpose(1, 0, 2).reshape(2, D)
    sums = jnp.concatenate(
        [sums_in[0:1], sums[1:2], sums_in[1:2], qv, sums[5:12]], 0
    )
    sums = lax.psum_scatter(sums, ("dp", "tensor"), scatter_dimension=1, tiled=True)
    return layer_out, tokens_grad, *placed(tie_map, sums, part0, part1, part2)


def fused_step(
    tokens, lengths, tie_map, norm_gains, bias_rows, attention_in, attention_out,
    expand_weight, project_weight, cotangent,
):
    slots = lengths.shape[0]
    tokens = tokens.reshape(slots, -1, D)
    cotangent = cotangent.reshape(slots, -1, D)
    gq, gw, g1, g2, rows, q, v, kt, p, scale, o, a1t, h1, a2, a2t = run_fused_forward(
        tie_map, lengths, tokens, norm_gains, bias_rows, attention_in, attention_out,
        expand_weight, project_weight,
    )
    layer, fold, work, dh1, gb, gbt, early = run_fused_feed_forward(
        lengths, cotangent, a2, a2t, h1, g1, g2, rows
    )
    grad, out, part0, partw, part1, part2, sums = run_fused_backward(
        tokens, gq, gw, rows, dh1, gb, gbt, q, v, kt, p, scale, o, a1t, layer, fold,
        work, early,
    )
    out, grad, *placed_grads = run_place_gradients(
        tie_map, sums, part0, partw, part1, part2, out, grad,
        (norm_gains, bias_rows, attention_in, attention_out, expand_weight, project_weight),
    )
    return out.reshape(-1, D), grad.reshape(-1, D), *placed_grads


def placed(tie_map, sums, part0, part1, part2):
    source = jnp.arange(NSRC, dtype=jnp.int32)

    def place(piece, which):
        pick = (source == tie_map[which]).reshape((NSRC,) + (1,) * piece.ndim)
        return jnp.where(pick, piece[None], 0.0)

    def place_rows(piece, kinds):
        pick = source[:, None] == tie_map[jnp.array(kinds, dtype=jnp.int32)][None, :]
        return jnp.where(pick[:, :, None], piece[None], 0.0)

    return (
        place_rows(sums[:2], [0, 2]),
        place_rows(sums[2:], [0, 0, 0, 1, 2, 3] + [2] * (FF // D)),
        place(part0[:3], 0),
        place(part0[3].T, 1),
        place(part1, 2),
        place(part2.T, 3),
    )


def solution(mesh):
    fused = mesh.shape["dp"] == Z_DEV * Y_DEV and mesh.shape["tensor"] == X_DEV * C_DEV
    return jax.shard_map(
        fused_step if fused else plain_step,
        mesh=mesh,
        in_specs=(
            P("dp", None),
            P("dp"),
            P(),
            P(None, None, ("dp", "tensor")),
            P(None, None, ("dp", "tensor")),
            P(None, None, "dp", "tensor"),
            P(None, "tensor", "dp"),
            P(None, "dp", "tensor"),
            P(None, "tensor", "dp"),
            P("dp", None),
        ),
        out_specs=(
            P("dp", None),
            P("dp", None),
            P(None, None, ("dp", "tensor")),
            P(None, None, ("dp", "tensor")),
            P(None, None, "dp", "tensor"),
            P(None, "tensor", "dp"),
            P(None, "dp", "tensor"),
            P(None, "tensor", "dp"),
        ),
        check_vma=False,
    )
```

```python
import jax
import jax.numpy as jnp
from jax import lax
from jax.experimental import pallas as pl
from jax.experimental.pallas import tpu as pltpu
from jax.sharding import PartitionSpec as P

D = 768
HEAD_DIM = 64
FF = 3072
NSRC = 4
EPS = 1e-05
MASKED = -1e30
F32 = jnp.float32
BF16 = jnp.bfloat16
VMEM_LIMIT = 60 * 1024 * 1024


def dot_nn(a, b):
    return lax.dot_general(a, b, (((1,), (0,)), ((), ())), preferred_element_type=F32)


def dot_nt(a, b):
    return lax.dot_general(a, b, (((1,), (1,)), ((), ())), preferred_element_type=F32)


def norm_parts(v):
    center = jnp.mean(v, -1, keepdims=True)
    centered = v - center
    r = lax.rsqrt(jnp.mean(centered * centered, -1, keepdims=True) + EPS)
    return centered * r, r


def head_mask(shape, h):
    lane = lax.broadcasted_iota(jnp.int32, shape, 1)
    return (lane >= h * HEAD_DIM) & (lane < (h + 1) * HEAD_DIM)


def blocks(total, size):
    return [slice(i * size, (i + 1) * size) for i in range(total // size)]


def attention_forward(
    len_ref, x_ref, g_ref, rows_ref, bqv_ref,
    q_ref, v_ref, kt_ref, p_ref, o_ref, a1t_ref, h1_ref, a2_ref, a2t_ref,
    a1_ref, k_ref, vt_ref, ot_ref, attn_ref,
):
    t = pl.program_id(0)
    n = x_ref.shape[0]
    width = g_ref.shape[-1]
    heads = width // HEAD_DIM
    step = 256
    length = len_ref[0]

    @pl.when(t == 0)
    def _():
        @pl.loop(0, n // step)
        def _(b):
            rows = pl.ds(pl.multiple_of(b * step, step), step)
            xhat, _ = norm_parts(x_ref[rows, :].astype(F32))
            a1 = xhat * rows_ref[0:1, :] + rows_ref[2:3, :]
            a1_ref[rows, :] = a1.astype(BF16)
            a1t_ref[:, rows] = a1.astype(BF16).T
            attn_ref[rows, :] = x_ref[rows, :].astype(F32) + rows_ref[5:6, :]

    @pl.loop(0, n // step)
    def _(b):
        rows = pl.ds(pl.multiple_of(b * step, step), step)
        a1 = a1_ref[rows, :]
        q = (dot_nn(a1, g_ref[0, 0]) + bqv_ref[0, 0:1, :]).astype(BF16)
        q_ref[0, rows, :] = q * jnp.asarray(HEAD_DIM ** -0.5, BF16)
        k = dot_nn(a1, g_ref[0, 1]).astype(BF16)
        k_ref[rows, :] = k
        kt_ref[0, :, rows] = k.T
        v = (dot_nn(a1, g_ref[0, 2]) + bqv_ref[0, 1:2, :]).astype(BF16)
        v_ref[0, rows, :] = v
        vt_ref[:, rows] = v.T

    for h in range(heads):
        k = k_ref[...]
        k = jnp.where(head_mask(k.shape, h), k, jnp.zeros_like(k))
        for b in range(n // step):
            first, last = b * step, (b + 1) * step
            q = q_ref[0, first:last, :]
            key = lax.broadcasted_iota(jnp.int32, (last, step), 0)
            query = lax.broadcasted_iota(jnp.int32, (step, step), 1) + first
            s = dot_nt(k[:last], q)
            near = jnp.where(
                (key[first:] <= query) & (key[first:] < length), s[first:], MASKED
            )
            if b:
                far = jnp.where(key[:first] < length, s[:first], MASKED)
                top = jnp.maximum(
                    jnp.max(far, 0, keepdims=True), jnp.max(near, 0, keepdims=True)
                )
                e_far = jnp.exp(far - top)
                e_near = jnp.exp(near - top)
                total = jnp.sum(e_far, 0, keepdims=True) + jnp.sum(e_near, 0, keepdims=True)
                scale = 1.0 / total
                p_ref[0, h, :first, first:last] = (e_far * scale).astype(BF16)
            else:
                top = jnp.max(near, 0, keepdims=True)
                e_near = jnp.exp(near - top)
                scale = 1.0 / jnp.sum(e_near, 0, keepdims=True)
            p_ref[0, h, first:last, first:last] = (e_near * scale).astype(BF16)
            ot_ref[h * HEAD_DIM : (h + 1) * HEAD_DIM, first:last] = dot_nn(
                vt_ref[h * HEAD_DIM : (h + 1) * HEAD_DIM, :last],
                p_ref[0, h, :last, first:last],
            ).astype(BF16)

    @pl.loop(0, n // step)
    def _(b):
        rows = pl.ds(pl.multiple_of(b * step, step), step)
        o = ot_ref[:, rows].T
        o_ref[0, rows, :] = o
        attn_ref[rows, :] += dot_nt(o, g_ref[0, 3])

    @pl.when(t == pl.num_programs(0) - 1)
    def _():
        @pl.loop(0, n // step)
        def _(b):
            rows = pl.ds(pl.multiple_of(b * step, step), step)
            h1 = attn_ref[rows, :]
            h1_ref[rows, :] = h1
            xhat, _ = norm_parts(h1)
            a2 = (xhat * rows_ref[1:2, :] + rows_ref[6:7, :]).astype(BF16)
            a2_ref[rows, :] = a2
            a2t_ref[:, rows] = a2.T


SQRT_2_PI = 0.7978845608028654


def feed_forward_both(
    len_ref, c_ref, a2_ref, a2t_ref, h1_ref, w1_ref, w2_ref, rows_ref,
    out_ref, d1_ref, d2_ref, dh1_ref, gb_ref, gbt_ref, sums_ref,
    gf_ref, gft_ref, feed_ref, da2_ref, h_ref, df_ref,
):
    t = pl.program_id(0)
    n = c_ref.shape[0]
    step = 256
    length = len_ref[0]

    @pl.when(t == 0)
    def _():
        sums_ref[...] = jnp.zeros_like(sums_ref)

        @pl.loop(0, n // step)
        def _(b):
            rows = pl.ds(pl.multiple_of(b * step, step), step)
            place = b * step + lax.broadcasted_iota(jnp.int32, (step, 1), 0)
            live = (place < length).astype(F32)
            g = (c_ref[rows, :].astype(F32) * live).astype(BF16)
            gf_ref[rows, :] = g
            gft_ref[:, rows] = g.T
            sums_ref[7:8, :] += jnp.sum(g.astype(F32), 0, keepdims=True)

    bias = rows_ref[pl.ds(8 + t, 1), :]

    @pl.loop(0, n // step)
    def _(b):
        rows = pl.ds(pl.multiple_of(b * step, step), step)
        f = dot_nn(a2_ref[rows, :], w1_ref[0]) + bias
        dh = dot_nn(gf_ref[rows, :], w2_ref[0])
        f2 = f * f
        th = jnp.tanh(f * (SQRT_2_PI + (SQRT_2_PI * 0.044715) * f2))
        half = 0.5 + 0.5 * th
        h = (f * half).astype(BF16)
        slope = half + f * (0.5 - 0.5 * th * th) * (
            SQRT_2_PI + (3 * SQRT_2_PI * 0.044715) * f2
        )
        df = (dh * slope).astype(BF16)
        h_ref[rows, :] = h
        df_ref[rows, :] = df
        sums_ref[pl.ds(8 + t, 1), :] += jnp.sum(df.astype(F32), 0, keepdims=True)
        feed = dot_nt(h, w2_ref[0])
        da2 = dot_nt(df, w1_ref[0])

        @pl.when(t == 0)
        def _():
            feed_ref[rows, :] = feed
            da2_ref[rows, :] = da2

        @pl.when(t > 0)
        def _():
            feed_ref[rows, :] += feed
            da2_ref[rows, :] += da2

    @pl.loop(0, D // step)
    def _(b):
        rows = pl.ds(pl.multiple_of(b * step, step), step)
        d1_ref[0, rows, :] = dot_nn(a2t_ref[rows, :], df_ref[...]).astype(BF16)
        d2_ref[0, rows, :] = dot_nn(gft_ref[rows, :], h_ref[...]).astype(BF16)

    @pl.when(t == pl.num_programs(0) - 1)
    def _():
        @pl.loop(0, n // step)
        def _(b):
            rows = pl.ds(pl.multiple_of(b * step, step), step)
            place = b * step + lax.broadcasted_iota(jnp.int32, (step, 1), 0)
            live = (place < length).astype(F32)
            h1 = h1_ref[rows, :]
            out_ref[rows, :] = (live * (h1 + (feed_ref[rows, :] + rows_ref[7:8, :]))).astype(BF16)
            xhat, r = norm_parts(h1)
            da2 = da2_ref[rows, :]
            sums_ref[1:2, :] += jnp.sum(da2 * xhat, 0, keepdims=True)
            sums_ref[6:7, :] += jnp.sum(da2, 0, keepdims=True)
            dg = da2 * rows_ref[1:2, :]
            dv = r * (
                dg
                - jnp.mean(dg, -1, keepdims=True)
                - xhat * jnp.mean(dg * xhat, -1, keepdims=True)
            )
            dh1 = live * c_ref[rows, :].astype(F32) + dv
            dh1_ref[rows, :] = dh1
            gb = dh1.astype(BF16)
            gb_ref[rows, :] = gb
            gbt_ref[:, rows] = gb.T
            sums_ref[5:6, :] += jnp.sum(gb.astype(F32), 0, keepdims=True)


def attention_backward(
    x_ref, g_ref, rows_ref, dh1_ref, gb_ref, gbt_ref, q_ref, v_ref, kt_ref, p_ref,
    o_ref, a1t_ref,
    d0_ref, xg_ref, sums_ref, bqv_ref,
    do_ref, delta_ref, dqt_ref, dq_ref, dk_ref, dv_ref, da1_ref,
):
    t = pl.program_id(0)
    n = x_ref.shape[0]
    width = g_ref.shape[-1]
    heads = width // HEAD_DIM
    step = 256
    pick = (
        lax.broadcasted_iota(jnp.int32, (16, width), 1) // HEAD_DIM
        == lax.broadcasted_iota(jnp.int32, (16, width), 0)
    ).astype(BF16)

    @pl.loop(0, n // step)
    def _(b):
        rows = pl.ds(pl.multiple_of(b * step, step), step)
        do = dot_nn(gb_ref[rows, :], g_ref[0, 3]).astype(BF16)
        do_ref[rows, :] = do
        prod = do.astype(F32) * o_ref[0, rows, :].astype(F32)
        high = prod.astype(BF16)
        low = (prod - high.astype(F32)).astype(BF16)
        delta_ref[:, rows] = dot_nt(pick, high) + dot_nt(pick, low)

    dqt_ref[...] = jnp.zeros_like(dqt_ref)
    for b in range(n // step):
        first, last = b * step, (b + 1) * step
        do = do_ref[first:, :]
        q = q_ref[0, first:, :]
        v = v_ref[0, first:last, :]
        dk, dv = None, None
        for h in range(heads):
            mine = head_mask((1, width), h)
            zero = jnp.zeros((), BF16)
            p = p_ref[0, h, first:last, first:]
            dp = dot_nt(jnp.where(mine, v, zero), do)
            ds = (p.astype(F32) * (dp - delta_ref[h : h + 1, first:])).astype(BF16)
            part = dot_nn(p, jnp.where(mine, do, zero))
            dv = part if dv is None else dv + part
            part = dot_nn(ds, jnp.where(mine, q, zero))
            dk = part if dk is None else dk + part
            head = slice(h * HEAD_DIM, (h + 1) * HEAD_DIM)
            dqt_ref[head, first:] += dot_nn(kt_ref[0, head, first:last], ds)
        dk_ref[first:last, :] = dk.astype(BF16)
        dv_ref[first:last, :] = dv.astype(BF16)

    @pl.when(t == 0)
    def _():
        da1_ref[...] = jnp.zeros_like(da1_ref)

    bqv_ref[...] = jnp.zeros_like(bqv_ref)

    @pl.loop(0, n // step)
    def _(b):
        rows = pl.ds(pl.multiple_of(b * step, step), step)
        dq = (dqt_ref[:, rows] * HEAD_DIM ** -0.5).astype(BF16).T
        dk = dk_ref[rows, :]
        dv = dv_ref[rows, :]
        dq_ref[rows, :] = dq
        bqv_ref[0, 0:1, :] += jnp.sum(dq.astype(F32), 0, keepdims=True)
        bqv_ref[0, 1:2, :] += jnp.sum(dv.astype(F32), 0, keepdims=True)
        da1_ref[rows, :] += (
            dot_nt(dq, g_ref[0, 0]) + dot_nt(dk, g_ref[0, 1]) + dot_nt(dv, g_ref[0, 2])
        )

    @pl.loop(0, D // step)
    def _(b):
        rows = pl.ds(pl.multiple_of(b * step, step), step)
        a1t = a1t_ref[rows, :]
        d0_ref[0, 0, rows, :] = dot_nn(a1t, dq_ref[...]).astype(BF16)
        d0_ref[0, 1, rows, :] = dot_nn(a1t, dk_ref[...]).astype(BF16)
        d0_ref[0, 2, rows, :] = dot_nn(a1t, dv_ref[...]).astype(BF16)
        d0_ref[0, 3, rows, :] = dot_nn(gbt_ref[rows, :], o_ref[0]).astype(BF16)

    @pl.when(t == pl.num_programs(0) - 1)
    def _():
        sums_ref[...] = jnp.zeros_like(sums_ref)

        @pl.loop(0, n // step)
        def _(b):
            rows = pl.ds(pl.multiple_of(b * step, step), step)
            xhat, r = norm_parts(x_ref[rows, :].astype(F32))
            da1 = da1_ref[rows, :]
            sums_ref[0:1, :] += jnp.sum(da1 * xhat, 0, keepdims=True)
            sums_ref[1:2, :] += jnp.sum(da1, 0, keepdims=True)
            dg = da1 * rows_ref[0:1, :]
            dv = r * (
                dg
                - jnp.mean(dg, -1, keepdims=True)
                - xhat * jnp.mean(dg * xhat, -1, keepdims=True)
            )
            xg_ref[rows, :] = (dh1_ref[rows, :] + dv).astype(BF16)


def whole(*shape):
    return pl.BlockSpec(shape, lambda t: (0,) * len(shape))


def group(*shape):
    return pl.BlockSpec((1,) + shape, lambda t: (t,) + (0,) * len(shape))


def shaped(dtype, *shape):
    return jax.ShapeDtypeStruct(shape, dtype)


SMEM_WHOLE = pl.BlockSpec(memory_space=pltpu.SMEM)


def run_attention_forward(length, x, g0, rows, bqv):
    n = x.shape[0]
    groups, _, _, width = g0.shape
    heads = width // HEAD_DIM
    return pl.pallas_call(
        attention_forward,
        grid=(groups,),
        in_specs=[SMEM_WHOLE, whole(n, D), group(4, D, width), whole(16, D), group(2, width)],
        out_specs=[
            group(n, width), group(n, width), group(width, n), group(heads, n, n),
            group(n, width), whole(D, n), whole(n, D), whole(n, D), whole(D, n),
        ],
        out_shape=[
            shaped(BF16, groups, n, width), shaped(BF16, groups, n, width),
            shaped(BF16, groups, width, n), shaped(BF16, groups, heads, n, n),
            shaped(BF16, groups, n, width), shaped(BF16, D, n), shaped(F32, n, D),
            shaped(BF16, n, D), shaped(BF16, D, n),
        ],
        scratch_shapes=[
            pltpu.VMEM((n, D), BF16), pltpu.VMEM((n, width), BF16),
            pltpu.VMEM((width, n), BF16), pltpu.VMEM((width, n), BF16),
            pltpu.VMEM((n, D), F32),
        ],
        compiler_params=pltpu.CompilerParams(vmem_limit_bytes=VMEM_LIMIT),
        name="attention_forward",
    )(length, x, g0, rows, bqv)


def run_feed_forward(length, cot, a2, a2t, h1, g1, g2, rows):
    n = cot.shape[0]
    groups, _, width = g1.shape
    return pl.pallas_call(
        feed_forward_both,
        grid=(groups,),
        in_specs=[
            SMEM_WHOLE, whole(n, D), whole(n, D), whole(D, n), whole(n, D),
            group(D, width), group(D, width), whole(16, D),
        ],
        out_specs=[
            whole(n, D), group(D, width), group(D, width), whole(n, D), whole(n, D),
            whole(D, n), whole(16, D),
        ],
        out_shape=[
            shaped(BF16, n, D), shaped(BF16, groups, D, width), shaped(BF16, groups, D, width),
            shaped(F32, n, D), shaped(BF16, n, D), shaped(BF16, D, n), shaped(F32, 16, D),
        ],
        scratch_shapes=[
            pltpu.VMEM((n, D), BF16), pltpu.VMEM((D, n), BF16), pltpu.VMEM((n, D), F32),
            pltpu.VMEM((n, D), F32), pltpu.VMEM((n, width), BF16), pltpu.VMEM((n, width), BF16),
        ],
        compiler_params=pltpu.CompilerParams(vmem_limit_bytes=VMEM_LIMIT),
        name="feed_forward_both",
    )(length, cot, a2, a2t, h1, g1, g2, rows)


def run_attention_backward(x, g0, rows, dh1, gb, gbt, q, v, kt, p, o, a1t):
    n = x.shape[0]
    groups, _, _, width = g0.shape
    heads = width // HEAD_DIM
    return pl.pallas_call(
        attention_backward,
        grid=(groups,),
        in_specs=[
            whole(n, D), group(4, D, width), whole(16, D), whole(n, D), whole(n, D),
            whole(D, n), group(n, width), group(n, width), group(width, n),
            group(heads, n, n), group(n, width), whole(D, n),
        ],
        out_specs=[group(4, D, width), whole(n, D), whole(8, D), group(8, width)],
        out_shape=[
            shaped(BF16, groups, 4, D, width), shaped(BF16, n, D), shaped(F32, 8, D),
            shaped(F32, groups, 8, width),
        ],
        scratch_shapes=[
            pltpu.VMEM((n, width), BF16), pltpu.VMEM((16, n), F32), pltpu.VMEM((width, n), F32),
            pltpu.VMEM((n, width), BF16), pltpu.VMEM((n, width), BF16),
            pltpu.VMEM((n, width), BF16), pltpu.VMEM((n, D), F32),
        ],
        compiler_params=pltpu.CompilerParams(vmem_limit_bytes=VMEM_LIMIT),
        name="attention_backward",
    )(x, g0, rows, dh1, gb, gbt, q, v, kt, p, o, a1t)


Z_DEV, Y_DEV, X_DEV, C_DEV = 4, 2, 2, 2


class Place:
    def __init__(self):
        dp, self.t = lax.axis_index("dp"), lax.axis_index("tensor")
        self.dp = dp
        self.z, self.y = dp // 2, dp % 2
        self.x, self.c = self.t // 2, self.t % 2
        self.other_y = 1 - self.y
        self.zs = [
            self.z,
            self.z + 1 - 2 * (self.z % 2),
            self.z + 2 - 4 * (self.z // 2),
            3 - self.z,
        ]
        self.ts = [
            self.t,
            self.t + 1 - 2 * (self.t % 2),
            self.t + 2 - 4 * (self.t // 2),
            3 - self.t,
        ]
        self.to_z = [dict(dp=z * 2 + self.y) for z in self.zs]
        self.to_y = dict(dp=self.z * 2 + self.other_y)
        self.to_x = dict(tensor=self.ts[2])
        self.same_t = self.to_z[1:] + [dict(dp=z * 2 + self.other_y) for z in self.zs]
        self.same_dp = [dict(tensor=t) for t in self.ts[1:]]
        self.to_core = dict(tensor=self.ts[1])

    def group(self, k):
        return lax.select(
            k == 0, self.ts[0],
            lax.select(k == 1, self.ts[1], lax.select(k == 2, self.ts[2], self.ts[3])),
        )

    def greet(self, others=None):
        barrier = pltpu.get_barrier_semaphore()
        others = others or self.to_z[1:] + [self.to_y, self.to_x, self.to_core]
        for device in others:
            pl.semaphore_signal(
                barrier, inc=1, device_id=device, device_id_type=pl.DeviceIdType.MESH
            )
        pl.semaphore_wait(barrier, len(others))


class Pieces:
    def __init__(self, whole, pieces):
        self.whole, self.pieces = whole, pieces

    def start(self):
        for piece in self.pieces:
            piece.start()

    def wait_recv(self):
        self.whole.wait_recv()

    def wait_send(self):
        self.whole.wait_send()


class Links:
    def __init__(self, send_sem, recv_sem):
        self.send_sem, self.recv_sem = send_sem, recv_sem
        self.copies = []

    def add(self, device, src, dst, parts=1, axis=0):
        number = len(self.copies)

        def make(src, dst):
            return pltpu.make_async_remote_copy(
                src_ref=src,
                dst_ref=dst,
                send_sem=self.send_sem.at[number],
                recv_sem=self.recv_sem.at[number],
                device_id=device,
                device_id_type=pl.DeviceIdType.MESH,
            )

        size = src.shape[axis] // parts
        cuts = [(slice(None),) * axis + (pl.ds(i * size, size),) for i in range(parts)]
        copy = Pieces(make(src, dst), [make(src.at[cut], dst.at[cut]) for cut in cuts])
        self.copies.append(copy)
        return copy

    def sent(self, *apart):
        for copy in self.copies:
            if all(copy is not other for other in apart):
                copy.wait_send()


def flat(copies):
    for item in copies:
        if isinstance(item, list):
            yield from flat(item)
        else:
            yield item


def start(*copies):
    for copy in flat(copies):
        copy.start()


def recv(*copies):
    for copy in flat(copies):
        copy.wait_recv()


class Gather:
    def __init__(self, links, place, own, full, order, single=True, last=True):
        every = slice(None)
        y, other = place.y, place.other_y

        def same(device, k, yy, to):
            return links.add(device, full(k, every, yy), full(to, every, yy), Z_DEV)

        def along_z(k, yy, block):
            here, passed = full(k, place.z, yy), full(k, place.zs[2], yy)
            return [
                links.add(place.to_z[1], block, here),
                links.add(place.to_z[2], block, here),
                links.add(place.to_z[1], passed, passed),
            ]

        if order != WHOLE:
            self.z = along_z(0, y, own)
        if order == X_Z_Y:
            self.first = [links.add(place.to_x, own, full(2, place.z, y), 2)]
            self.far = along_z(2, y, full(2, place.z, y))
            blocks = [(0, y), (2, y), (0, other), (2, other)]
        else:
            blocks = [(0, y), (0, other), (2, y), (2, other)]
        if order == Y_Z_X:
            self.first = [links.add(place.to_y, own, full(0, place.z, y), 2)]
            self.far = along_z(0, other, full(0, place.z, other))
        if order == Z_Y_X and single:
            self.first = [same(place.to_y, 0, y, 0)]
        if order == Z_Y_X and not single:
            self.first = [links.add(place.to_y, own, full(0, place.z, y))]
            for k in range(1, 4):
                block = full(0, place.zs[k], y)
                self.first.append(links.add(place.to_y, block, block))
            return
        self.second = [
            same(place.to_y, k, yy, k) if order == X_Z_Y else same(place.to_x, k, yy, 2)
            for k, yy in blocks[: 2 if last else 1]
        ]
        if not last:
            blocks = [block for block in blocks if block[0] == 0]
        self.core = [same(place.to_core, k, yy, k + 1) for k, yy in blocks]


Z_Y_X, Y_Z_X, X_Z_Y, WHOLE = range(4)


def fused_forward(
    tie_ref, len_ref, tokens_ref, gains_ref, bias_ref, in_ref, out_ref, expand_ref,
    project_ref,
    gq_ref, gw_ref, flat1_ref, flat2_ref, rows_ref,
    q_ref, v_ref, kt_ref, p_ref, scale_ref, o_ref, a1t_out, h1_out, a2_out, a2t_out,
    own0_ref, ownw_ref, own1_ref, own2_ref, square_ref, vec_ref,
    all0_ref, allw_ref, w1_ref, w2_ref, vecs_ref, bqv_ref, x_ref, a1_ref, k_ref, qa_ref, vt_ref, ot_ref, a1t_ref, h1_ref, a2_ref, a2t_ref,
    send_sem, recv_sem, local_sem, flush_sem, row_sem,
):
    t, h = pl.program_id(0), pl.program_id(1)
    n, _ = x_ref.shape
    width = allw_ref.shape[-1]
    heads = width // HEAD_DIM
    step = 256
    place = Place()
    length = len_ref[place.t]
    links = Links(send_sem, recv_sem)
    z, y, x, c = place.z, place.y, place.x, place.c
    mine_there = vecs_ref.at[z, y, x, c]
    column = vecs_ref.at[:, :, x, c]
    vec_one = [links.add(device, vec_ref, mine_there) for device in place.same_t]
    vec_two = [links.add(device, column, column) for device in place.same_dp]
    half = own0_ref.shape[0] // 2
    halves = []
    for i in range(2):
        rows = pl.ds(i * half, half)
        halves.append(Gather(
            links, place, own0_ref.at[rows],
            lambda k, z, y, rows=rows: all0_ref.at[k, z, y, rows], Z_Y_X, single=False,
        ))
    seg0 = Gather(links, place, own0_ref, lambda k, z, y: all0_ref.at[k, z, y], WHOLE)
    segw = Gather(links, place, ownw_ref, lambda k, z, y: allw_ref.at[k, z, y], Z_Y_X)
    seg1 = Gather(
        links, place, own1_ref, lambda k, z, y: w1_ref.at[k, z, y], Y_Z_X, last=False
    )
    seg2 = Gather(
        links, place, own2_ref, lambda k, z, y: w2_ref.at[k, z, y], X_Z_Y, last=False
    )
    flush = [
        [
            pltpu.make_async_copy(ref.at[k], flat.at[k], flush_sem.at[i, k])
            for k in range(3)
        ]
        for i, (ref, flat) in enumerate([(w1_ref, flat1_ref), (w2_ref, flat2_ref)])
    ]
    put_a1t = pltpu.make_async_copy(a1t_ref, a1t_out, local_sem.at[0])
    put_a2t = pltpu.make_async_copy(a2t_ref, a2t_out, local_sem.at[1])
    puts = []
    for i in range(n // step):
        rows = pl.ds(i * step, step)
        puts.append([
            pltpu.make_async_copy(h1_ref.at[rows], h1_out.at[rows], row_sem.at[0, i]),
            pltpu.make_async_copy(a2_ref.at[rows], a2_out.at[rows], row_sem.at[1, i]),
        ])
    fetch = pltpu.make_async_copy(tokens_ref.at[place.t], x_ref, local_sem.at[2])

    def relay_z(copies):
        recv(copies[1])
        start(copies[2])

    def pass_own(seg):
        recv(seg.z[0], seg.z[2])
        if seg is segw:
            start(seg.first)
        start(seg.second[0], seg.core[0])

    def pass_second(seg):
        recv(seg.second)
        if seg is seg2:
            start(seg.core[1])

    def pass_first(seg):
        recv(seg.first)
        if seg is segw:
            start(seg.second[1], seg.core[1])
        else:
            start(seg.far[1], seg.far[0])

    def pass_far(seg):
        recv(seg.far[0], seg.far[2])
        start(seg.core[1:] if seg is seg1 else [])

    def pass_core(seg, i):
        recv(seg.second[i])
        start(seg.core[2 + i])

    plan = [
        (0, 0, lambda: (pass_own(segw), pass_first(seg1), relay_z(seg2.z), pass_first(seg2))),
        (0, 3, lambda: (pass_first(segw), relay_z(seg1.z), pass_core(seg0, 0))),
        (1, 0, lambda: recv(seg0.core[:2])),
        (1, 1, lambda: relay_z(seg1.far)),
        (1, 3, lambda: pass_core(seg0, 1)),
        (1, 4, lambda: (recv(segw.core[:2]), pass_core(segw, 0), pass_own(seg2))),
        (2, 1, lambda: relay_z(seg2.far)),
        (2, 2, lambda: pass_core(segw, 1)),
        (2, 3, lambda: pass_own(seg1)),
        (3, 0, lambda: (recv(seg0.core[2:]), pass_far(seg1), flush[0][0].start())),
        (3, 2, lambda: (pass_second(seg2), flush[1][0].start())),
        (3, 3, lambda: (pass_far(seg2), flush[1][2].start())),
        (3, 4, lambda: recv(segw.core[2:])),
    ]

    def serve(points):
        for step, where, act in plan:
            if where in points:
                now = (t == step) & (h == max(where - 2, 0))
                pl.when(now)(lambda act=act: (act(), None)[1])

    @pl.when((t == 0) & (h == 0))
    def _():
        s0, s1, s2, s3 = tie_ref[0], tie_ref[1], tie_ref[2], tie_ref[3]
        fetch.start()
        square_ref[...] = jnp.zeros_like(square_ref)
        gain = gains_ref.shape[-1]
        square_ref[0:1, :gain] = gains_ref[s0].astype(F32)[0:1]
        square_ref[1:2, :gain] = gains_ref[s2].astype(F32)[1:2]
        kinds = [s0, s0, s0, s1, s2, s3, s2, s2, s2, s2]
        for i, source in enumerate(kinds):
            wide = bias_ref[i].astype(F32)
            here = lax.broadcasted_iota(jnp.int32, wide.shape, 0) == source
            square_ref[2 + i : 3 + i, :gain] = jnp.sum(
                jnp.where(here, wide, 0.0), 0, keepdims=True
            )
        vec_ref[...] = square_ref[...].T[:gain]
        for j in range(3):
            own0_ref[:, j * width : (j + 1) * width] = in_ref[s0, j]
        place.greet(place.same_t + place.same_dp)
        start(vec_one)
        for part in halves:
            start(part.z[1], part.z[0], part.first[0])
        vecs_ref[z, y, x, c] = vec_ref[...]
        ones = lax.broadcasted_iota(jnp.int32, (vt_ref.shape[1] - HEAD_DIM, n), 0) == 0
        for h in range(heads):
            vt_ref[h, HEAD_DIM:, :] = ones.astype(BF16)
        all0_ref[0, z, y] = own0_ref[...]
        ownw_ref[...] = out_ref[s1].T
        allw_ref[0, z, y] = ownw_ref[...]
        own1_ref[...] = expand_ref[s2]
        own2_ref[...] = project_ref[s3]
        w1_ref[0, z, y] = own1_ref[...]
        w2_ref[0, z, y] = own2_ref[...]
        recv(vec_one)
        start(vec_two)
        for part in halves:
            relay_z(part.z)
            start(part.first[2])
        for part in halves:
            recv(part.z[0])
            start(part.first[1])
        start(segw.z[1], segw.z[0], seg2.z[1])
        recv(vec_two)
        start(seg2.first)
        vecs = vecs_ref[...].reshape(D, vecs_ref.shape[-1]).T[:16]
        rows_ref[...] = vecs
        for part in halves:
            recv(part.z[2])
            start(part.first[3])
        start(seg1.first, seg0.second[0], seg0.core[0])
        for k in range(4):
            part = slice(k * width, (k + 1) * width)
            bqv_ref[k, 0:1, :width] = vecs[3:4, part]
            bqv_ref[k, 0:1, width : 2 * width] = jnp.zeros((1, width), F32)
            bqv_ref[k, 0:1, 2 * width :] = vecs[4:5, part]
        fetch.wait()

        @pl.loop(0, n // step)
        def _(b):
            rows = pl.ds(pl.multiple_of(b * step, step), step)
            wide = x_ref[rows, :].astype(F32)
            xhat, _ = norm_parts(wide)
            a1 = (xhat * rows_ref[0:1, :] + rows_ref[2:3, :]).astype(BF16)
            a1_ref[rows, :] = a1
            a1t_ref[:, rows] = a1.T
            h1_ref[rows, :] = wide + rows_ref[5:6, :]

        put_a1t.start()
        relay_z(segw.z)
        start(seg2.z[0], seg1.z[1], seg1.z[0])
        recv(halves[0].first, halves[1].first)
        start(seg0.second[1], seg0.core[1])

    serve([0])

    @pl.when(h == 0)
    def _():
        gq = all0_ref[t].reshape(D, 3 * width)
        gq_ref[0] = gq
        mine = place.group(t)
        qkv = dot_nn(a1_ref[...], gq) + bqv_ref[mine, 0:1, :]
        q = qkv[:, :width].astype(BF16) * jnp.asarray(HEAD_DIM ** -0.5, BF16)
        k = qkv[:, width : 2 * width].astype(BF16)
        v = qkv[:, 2 * width :].astype(BF16)
        q_ref[0] = q
        kt_ref[0] = k.T
        v_ref[0] = v
        vt = v.T
        for h in range(heads):
            vt_ref[h, :HEAD_DIM, :] = vt[h * HEAD_DIM : (h + 1) * HEAD_DIM]
        spare = k_ref.shape[1] - width
        dead = lax.broadcasted_iota(jnp.int32, (n, spare), 0) >= length
        first_column = lax.broadcasted_iota(jnp.int32, (n, spare), 1) == 0
        k_ref[:, :width] = k
        k_ref[:, width:] = jnp.where(first_column & dead, MASKED, 0.0).astype(BF16)
        qa_ref[:, :width] = q
        qa_ref[:, width:] = jnp.where(first_column, 1.0, 0.0).astype(BF16)
        scale_ref[0, heads:, :] = jnp.zeros((scale_ref.shape[1] - heads, n), F32)

    serve([1])

    lane = lax.broadcasted_iota(jnp.int32, (1, qa_ref.shape[1]), 1)
    keep = ((lane >= h * HEAD_DIM) & (lane < (h + 1) * HEAD_DIM)) | (lane >= width)
    key = lax.broadcasted_iota(jnp.int32, (step, step), 0)
    query = lax.broadcasted_iota(jnp.int32, (step, step), 1)
    head = pl.ds(pl.multiple_of(h * HEAD_DIM, HEAD_DIM), HEAD_DIM)

    def scores(b):
        first, last = b * step, (b + 1) * step
        q = jnp.where(keep, qa_ref[first:last, :], jnp.zeros((), BF16))
        return dot_nt(k_ref[:last, :], q)

    def attend(b, s):
        first, last = b * step, (b + 1) * step
        near = jnp.where(key <= query, s[first:], MASKED)
        top = jnp.max(near, 0, keepdims=True)
        if b:
            far = s[:first]
            top = jnp.maximum(top, jnp.max(far, 0, keepdims=True))
        e_near = jnp.exp((near - top).astype(BF16))
        p_ref[0, 0, b, first:last, :] = e_near
        o = dot_nn(vt_ref[h, :, first:last], e_near)
        if b:
            e_far = jnp.exp((far - top).astype(BF16))
            p_ref[0, 0, b, :first, :] = e_far
            o += dot_nn(vt_ref[h, :, :first], e_far)
        scale = 1.0 / o[HEAD_DIM : HEAD_DIM + 1]
        scale_ref[0, pl.ds(h, 1), first:last] = scale
        ot_ref[head, first:last] = (o[:HEAD_DIM] * scale).astype(BF16)

    s = scores(0)
    for b in range(n // step):
        ahead = scores(b + 1) if b + 1 < n // step else None
        attend(b, s)
        s = ahead

    serve([2, 3, 4])

    @pl.when(h == heads - 1)
    def _():
        gw_ref[0] = allw_ref[t].reshape(gw_ref.shape[1:])
        o = ot_ref[...].T
        o_ref[0] = o
        h1_ref[...] += dot_nt(o, gw_ref[0])

    @pl.when((t == 3) & (h == heads - 1))
    def _():
        for i, rows in enumerate(blocks(n, step)):
            xhat, _ = norm_parts(h1_ref[rows, :])
            a2 = (xhat * rows_ref[1:2, :] + rows_ref[6:7, :]).astype(BF16)
            a2_ref[rows, :] = a2
            a2t_ref[:, rows] = a2.T
            for put in puts[i]:
                put.start()
        put_a2t.start()
        recv(seg2.core)
        flush[1][1].start()
        recv(seg1.core)
        flush[0][1].start()
        pass_second(seg1)
        flush[0][2].start()
        links.sent()
        for copies in flush + puts + [[put_a1t, put_a2t]]:
            for copy in copies:
                copy.wait()


N_GATHER = 10 + 14 + 6 + 10 + 10 + 10
VMEM_WHOLE = pl.BlockSpec(memory_space=pltpu.VMEM)
ANY_WHOLE = pl.BlockSpec(memory_space=pl.ANY)


def run_fused_forward(tie, lengths, tokens, gains, biases, w_in, w_out, w_expand, w_project):
    groups, n, _ = tokens.shape
    depth, width = w_in.shape[-2:]
    heads = width // HEAD_DIM
    hidden = w_expand.shape[-1]
    w_project = w_project.transpose(0, 2, 1)
    biases = biases.transpose(1, 0, 2)
    own = gains.shape[-1]

    def group(*shape):
        return pl.BlockSpec((1,) + shape, lambda t, h: (t,) + (0,) * len(shape))

    per_head = pl.BlockSpec((1, 1, n // 256, n, 256), lambda t, h: (t, h, 0, 0, 0))
    return pl.pallas_call(
        fused_forward,
        grid=(groups, heads),
        in_specs=[SMEM_WHOLE, SMEM_WHOLE, ANY_WHOLE] + [VMEM_WHOLE] * 6,
        out_specs=[
            group(D, 3 * width), group(D, width), ANY_WHOLE, ANY_WHOLE, VMEM_WHOLE,
            group(n, width), group(n, width), group(width, n), per_head,
            group(8, n), group(n, width), ANY_WHOLE, ANY_WHOLE, ANY_WHOLE, ANY_WHOLE,
        ],
        out_shape=[
            shaped(BF16, groups, D, 3 * width), shaped(BF16, groups, D, width),
            shaped(BF16, groups, Z_DEV, Y_DEV, depth, hidden),
            shaped(BF16, groups, Z_DEV, Y_DEV, depth, hidden),
            shaped(F32, 16, D),
            shaped(BF16, groups, n, width), shaped(BF16, groups, n, width),
            shaped(BF16, groups, width, n), shaped(BF16, groups, heads, n // 256, n, 256),
            shaped(F32, groups, 8, n), shaped(BF16, groups, n, width), shaped(BF16, D, n), shaped(F32, n, D),
            shaped(BF16, n, D), shaped(BF16, D, n),
        ],
        scratch_shapes=[
            pltpu.VMEM((depth, 3 * width), BF16), pltpu.VMEM((depth, width), BF16),
            pltpu.VMEM((depth, hidden), BF16), pltpu.VMEM((depth, hidden), BF16),
            pltpu.VMEM((128, 128), F32), pltpu.VMEM((own, 128), F32),
            pltpu.VMEM((groups, Z_DEV, Y_DEV, depth, 3 * width), BF16),
            pltpu.VMEM((groups, Z_DEV, Y_DEV, depth, width), BF16),
            pltpu.VMEM((groups, Z_DEV, Y_DEV, depth, hidden), BF16),
            pltpu.VMEM((groups, Z_DEV, Y_DEV, depth, hidden), BF16),
            pltpu.VMEM((Z_DEV, Y_DEV, X_DEV, C_DEV, own, 128), F32),
            pltpu.VMEM((groups, 8, 3 * width), F32),
            pltpu.VMEM((n, D), BF16), pltpu.VMEM((n, D), BF16), pltpu.VMEM((n, 256), BF16),
            pltpu.VMEM((n, 256), BF16), pltpu.VMEM((heads, HEAD_DIM + 16, n), BF16),
            pltpu.VMEM((width, n), BF16),
            pltpu.VMEM((D, n), BF16), pltpu.VMEM((n, D), F32), pltpu.VMEM((n, D), BF16),
            pltpu.VMEM((D, n), BF16),
            pltpu.SemaphoreType.DMA((N_GATHER,)), pltpu.SemaphoreType.DMA((N_GATHER,)),
            pltpu.SemaphoreType.DMA((3,)), pltpu.SemaphoreType.DMA((2, 4)),
            pltpu.SemaphoreType.DMA((2, n // 256)),
        ],
        compiler_params=pltpu.CompilerParams(
            vmem_limit_bytes=VMEM_LIMIT, collective_id=0, has_side_effects=True
        ),
        name="fused_forward",
    )(tie, lengths, tokens, gains, biases, w_in, w_out, w_expand, w_project)


class Result:
    def __init__(self, links, place, own_ref, passing_ref, out_ref, step, sem, count):
        self.x, self.core, self.far, self.keep, self.keep_far = [], [], [], [], []
        for i in range(count):
            rows = pl.ds(i * step, step)
            mine, theirs = out_ref.at[place.t, rows], out_ref.at[place.ts[2], rows]
            own, passing = own_ref.at[rows], passing_ref.at[rows]
            self.x.append(links.add(place.to_x, own, passing))
            self.core.append(links.add(place.to_core, own, mine))
            self.far.append(links.add(place.to_core, passing, theirs))
            self.keep.append(pltpu.make_async_copy(own, mine, sem.at[0, i]))
            self.keep_far.append(pltpu.make_async_copy(passing, theirs, sem.at[1, i]))

    def send(self, i):
        start(self.x[i], self.core[i], self.keep[i])

    def pass_on(self, i):
        recv(self.x[i])
        start(self.far[i], self.keep_far[i])

    def finish(self):
        recv(self.core, self.far)
        for copy in self.keep + self.keep_far:
            copy.wait()


def low(value):
    return jnp.asarray(value, BF16)


def pair_order(i):
    return i + 1 - 2 * (i % 2)


def fused_feed_forward(
    len_ref, cot_ref, a2_ref, a2t_in, h1_in, far1_ref, far2_ref, rows_ref,
    out_out, fold_ref, work_out, dh1_out, gb_out, gbt_out, sums_ref,
    gf_ref, gft_ref, feed_ref, da2_ref, h_ref, df_ref, weights_ref, missing_ref, third_ref,
    stage_ref, land_ref, near_ref, cross_ref, a2t_ref, h1_ref, out_ref, work_ref,
    send_sem, recv_sem, local_sem, row_sem,
):
    t = pl.program_id(0)
    n = gf_ref.shape[0]
    step = 256
    depth = stage_ref.shape[-2]
    place = Place()
    length = len_ref[place.t]
    links = Links(send_sem, recv_sem)
    y, other = place.y, place.other_y
    last = [
        links.add(place.to_x, far1_ref.at[0, :, other], missing_ref.at[0, 0]),
        links.add(place.to_y, far2_ref.at[2, :, y], missing_ref.at[1, 0]),
    ]
    last_core = [
        links.add(place.to_core, missing_ref.at[i, 0], missing_ref.at[i, 1]) for i in range(2)
    ]
    third = [
        links.add(place.to_core, far_ref.at[2, :, y], third_ref.at[i])
        for i, far_ref in enumerate([far1_ref, far2_ref])
    ]
    core = [
        [links.add(place.to_core, stage_ref.at[i], land_ref.at[s, i]) for i in range(2)]
        for s in range(2)
    ]
    cross = [
        links.add(place.to_y, near_ref.at[i, :, other], cross_ref.at[i]) for i in range(2)
    ]
    fetch = pltpu.make_async_copy(cot_ref.at[place.t], gf_ref, local_sem.at[0])
    gb_ref, gbt_ref, dh1_ref = gf_ref, gft_ref, da2_ref
    late = [
        pltpu.make_async_copy(a2t_in, a2t_ref, local_sem.at[5]),
        pltpu.make_async_copy(h1_in, h1_ref, local_sem.at[6]),
    ]
    puts = []
    for i in range(n // step):
        rows = pl.ds(i * step, step)
        puts.append([
            pltpu.make_async_copy(ref.at[rows], out.at[rows], row_sem.at[j, i])
            for j, (ref, out) in enumerate(
                [(out_ref, out_out), (dh1_ref, dh1_out), (gb_ref, gb_out)]
            )
        ])
    put_gbt = pltpu.make_async_copy(gbt_ref, gbt_out, local_sem.at[7])
    put_work = pltpu.make_async_copy(work_ref, work_out, local_sem.at[8])
    k = pair_order(t)
    mine = place.group(k)

    def load(step, whole, slot):
        for i, far_ref in enumerate([far1_ref, far2_ref]):
            group = far_ref.at[pair_order(step)]
            to = weights_ref.at[slot, i]
            if not whole:
                group, to = group.at[:, y], to.at[:, y]
            yield pltpu.make_async_copy(group, to, local_sem.at[1 + 2 * slot + i])

    def live_rows(b):
        at = b * step + lax.broadcasted_iota(jnp.int32, (step, 1), 0)
        return (at < length).astype(F32)

    @pl.when(t == 0)
    def _():
        fetch.start()
        for copy in load(0, True, 0):
            copy.start()
        for copy in late:
            copy.start()
        place.greet()
        start(last, third)
        sums_ref[...] = jnp.zeros_like(sums_ref)
        feed_ref[...] = jnp.zeros_like(feed_ref)
        da2_ref[...] = jnp.zeros_like(da2_ref)
        fetch.wait()

        @pl.loop(0, n // step)
        def _(b):
            rows = pl.ds(pl.multiple_of(b * step, step), step)
            g = (gf_ref[rows, :].astype(F32) * live_rows(b)).astype(BF16)
            gf_ref[rows, :] = g
            gft_ref[:, rows] = g.T
            sums_ref[7:8, :] += jnp.sum(g.astype(F32), 0, keepdims=True)

    for i in range(4):
        @pl.when(t == i)
        def _():
            if i == 2:
                recv(last_core, third)
            else:
                for copy in load(i, i < 2, i % 2):
                    copy.wait()
            if i in (0, 2):
                for copy in load(i + 1, i + 1 < 2, (i + 1) % 2):
                    copy.start()
            for j in range(2):
                if i == 2:
                    weights_ref[0, j, :, y] = third_ref[j]
                if i >= 2:
                    weights_ref[i % 2, j, :, other] = missing_ref[j, 3 - i]

    bias = rows_ref[pl.ds(8 + mine, 1), :]
    w1 = weights_ref[t % 2, 0].reshape(D, -1)
    w2 = weights_ref[t % 2, 1].reshape(D, -1)
    column = jnp.zeros((1, w1.shape[1]), F32)
    for rows in blocks(n, step):
        f = (dot_nn(a2_ref[rows, :], w1) + bias).astype(BF16)
        dh = dot_nn(gf_ref[rows, :], w2)
        f2 = f * f
        th = jnp.tanh(f * (low(SQRT_2_PI) + low(SQRT_2_PI * 0.044715) * f2))
        half = low(0.5) + low(0.5) * th
        h = f * half
        slope = half + f * (low(0.5) - low(0.5) * th * th) * (
            low(SQRT_2_PI) + low(3 * SQRT_2_PI * 0.044715) * f2
        )
        df = (dh * slope.astype(F32)).astype(BF16)
        h_ref[rows, :] = h
        df_ref[rows, :] = df
        column += jnp.sum(df.astype(F32), 0, keepdims=True)
        feed_ref[rows, :] += dot_nt(h, w2)
        da2_ref[rows, :] += dot_nt(df, w1)
    sums_ref[pl.ds(8 + mine, 1), :] = column

    @pl.when(t == 1)
    def _():
        recv(last)
        start(last_core)

    @pl.when(t == 0)
    def _():
        late[0].wait()

    def weight_grad(left_ref, right_ref):
        value = dot_nn(left_ref[...], right_ref[...])
        return value.reshape(Z_DEV, Y_DEV, depth, value.shape[-1]).astype(BF16)

    grad1 = weight_grad(a2t_ref, df_ref)
    grad2 = weight_grad(gft_ref, h_ref)

    def put(ref):
        ref[0] = grad1
        ref[1] = grad2

    def reduced(ref):
        return lambda i, s, z: (
            ref[i, z].astype(F32) + land_ref[s, i, z].astype(F32)
        ).astype(BF16)

    @pl.when(t == 0)
    def _():
        put(stage_ref)
        start(core[0])

    @pl.when(t == 1)
    def _():
        put(near_ref)
        recv(core[0])

        @pl.loop(0, Z_DEV)
        def _(z):
            for i in range(2):
                near_ref[i, z] = reduced(near_ref)(i, 0, z)

        start(cross)

    @pl.when(t == 2)
    def _():
        for copy in core[0]:
            copy.wait_send()
        put(stage_ref)
        start(core[1])

    @pl.when(t == 3)
    def _():
        put(work_ref)
        late[1].wait()
        for i, rows in enumerate(blocks(n, step)):
            live = live_rows(i)
            h1 = h1_ref[rows, :]
            out_ref[rows, :] = (live * (h1 + (feed_ref[rows, :] + rows_ref[7:8, :]))).astype(BF16)
            xhat, r = norm_parts(h1)
            da2 = da2_ref[rows, :]
            sums_ref[1:2, :] += jnp.sum(da2 * xhat, 0, keepdims=True)
            sums_ref[6:7, :] += jnp.sum(da2, 0, keepdims=True)
            dg = da2 * rows_ref[1:2, :]
            dv = r * (
                dg
                - jnp.mean(dg, -1, keepdims=True)
                - xhat * jnp.mean(dg * xhat, -1, keepdims=True)
            )
            dh1 = gf_ref[rows, :].astype(F32) + dv
            dh1_ref[rows, :] = dh1
            gb = dh1.astype(BF16)
            gb_ref[rows, :] = gb
            gbt_ref[:, rows] = gb.T
            sums_ref[5:6, :] += jnp.sum(gb.astype(F32), 0, keepdims=True)
            for copy in puts[i]:
                copy.start()
        put_gbt.start()
        recv(core[1])

        @pl.loop(0, Z_DEV)
        def _(z):
            for i in range(2):
                work_ref[i, z] = reduced(work_ref)(i, 1, z)

        put_work.start()
        recv(cross)

        @pl.loop(0, Z_DEV)
        def _(z):
            for i in range(2):
                fold_ref[i, z] = (
                    near_ref[i, z, y].astype(F32) + cross_ref[i, z].astype(F32)
                ).astype(BF16)

        links.sent(*core[0])
        for copies in puts + [[put_gbt, put_work]]:
            for copy in copies:
                copy.wait()


def run_fused_feed_forward(lengths, cot, a2, a2t, h1, g1, g2, rows):
    n = cot.shape[1]
    groups, _, _, depth, hidden = g1.shape
    both = (2, Z_DEV, Y_DEV, depth, hidden)
    fold = (2, Z_DEV, depth, hidden)
    return pl.pallas_call(
        fused_feed_forward,
        grid=(groups,),
        in_specs=[SMEM_WHOLE, ANY_WHOLE, VMEM_WHOLE] + [ANY_WHOLE] * 4 + [VMEM_WHOLE],
        out_specs=[ANY_WHOLE, VMEM_WHOLE] + [ANY_WHOLE] * 4 + [VMEM_WHOLE],
        out_shape=[
            shaped(BF16, n, D), shaped(BF16, *fold), shaped(BF16, *both), shaped(F32, n, D),
            shaped(BF16, n, D), shaped(BF16, D, n), shaped(F32, 16, D),
        ],
        scratch_shapes=[
            pltpu.VMEM((n, D), BF16), pltpu.VMEM((D, n), BF16), pltpu.VMEM((n, D), F32),
            pltpu.VMEM((n, D), F32), pltpu.VMEM((n, hidden), BF16), pltpu.VMEM((n, hidden), BF16),
            pltpu.VMEM((2,) + both, BF16),
            pltpu.VMEM((2,) + fold, BF16), pltpu.VMEM(fold, BF16), pltpu.VMEM(both, BF16),
            pltpu.VMEM((2,) + both, BF16),
            pltpu.VMEM(both, BF16), pltpu.VMEM(fold, BF16),
            pltpu.VMEM((D, n), BF16), pltpu.VMEM((n, D), F32), pltpu.VMEM((n, D), BF16),
            pltpu.VMEM(both, BF16),
            pltpu.SemaphoreType.DMA((12,)), pltpu.SemaphoreType.DMA((12,)),
            pltpu.SemaphoreType.DMA((9,)), pltpu.SemaphoreType.DMA((3, n // 256)),
        ],
        compiler_params=pltpu.CompilerParams(
            vmem_limit_bytes=VMEM_LIMIT, collective_id=1, has_side_effects=True
        ),
        name="fused_feed_forward",
    )(lengths, cot, a2, a2t, h1, g1, g2, rows)
class Reduce:
    def __init__(
        self, links, place, work, acc, cross_ref, far_ref, mid_ref, last_ref, side_ref,
        slots=(0, 1),
    ):
        self.place, self.work, self.acc = place, work, acc
        self.cross_ref, self.far_ref, self.mid_ref = cross_ref, far_ref, mid_ref
        self.last_ref, self.side_ref = last_ref, side_ref
        zs = place.zs
        self.y = {
            s: [
                links.add(
                    place.to_y, work(s, zs[j], place.other_y), cross_ref.at[s, zs[j]]
                )
                for j in (1, 3, 2, 0)
            ]
            for s in slots
        }
        self.z = [
            [
                links.add(place.to_z[1], acc(s, zs[1]), far_ref.at[s, 0]),
                links.add(place.to_z[1], acc(s, zs[3]), far_ref.at[s, 1]),
                links.add(place.to_z[2], mid_ref.at[s, 1], far_ref.at[s, 2]),
            ]
            for s in range(2)
        ]
        self.x = links.add(place.to_x, last_ref, side_ref)

    def fold_y(self, s, half):
        for i, j in [(0, 1), (1, 3), (2, 2), (3, 0)][2 * half : 2 * half + 2]:
            z = self.place.zs[j]
            recv(self.y[s][i])
            value = self.work(s, z, self.place.y)[...].astype(F32)
            self.acc(s, z)[...] = (value + self.cross_ref[s, z].astype(F32)).astype(BF16)
            if i < 2:
                start(self.z[s][i])

    def fold_z(self, s):
        recv(self.z[s][:2])
        for i in (1, 0):
            value = self.acc(s, self.place.zs[2 * i])[...].astype(F32)
            self.mid_ref[s, i] = (value + self.far_ref[s, i].astype(F32)).astype(BF16)
            if i:
                start(self.z[s][2])

    def own(self, s):
        recv(self.z[s][2])
        return self.mid_ref[s, 0].astype(F32) + self.far_ref[s, 2].astype(F32)

    def send_x(self):
        self.last_ref[...] = self.own(1).astype(BF16)
        start(self.x)

    def total(self):
        value = self.own(0)
        recv(self.x)
        return value + self.side_ref[...].astype(F32)


def fused_backward(
    tokens_ref, gq_in, gw_in, rows_ref, dh1_ref, gb_ref, gbt_in, q_in, v_in, kt_in,
    p_ref, scale_in, o_in, a1t_in, layer_in, fold_in, work_in, early_ref,
    out_ref, layerout_ref, part0_ref, partw_ref, part1_ref, part2_ref, total_ref,
    gq_ref, gw_ref, q_ref, v_ref, kt_ref, scale_ref, o_ref,
    a1t_ref, gbt_ref, layer_ref, fold_ref, work_ref, do_ref, delta_ref, dkv_ref, dqkv_ref, da1_ref, own_ref, passing_ref, passlayer_ref, bqv_ref,
    folded_ref, cross1_ref, far1_ref, mid1_ref, last1_ref, side1_ref,
    cross2_ref, far2_ref, mid2_ref, last2_ref, side2_ref,
    stagew_ref, landw_ref, workw_ref, crossw_ref, farw_ref, midw_ref, lastw_ref, sidew_ref,
    stage0_ref, land0_ref, work0_ref, cross0_ref, far0_ref, mid0_ref, last0_ref, side0_ref,
    sums_ref, sumland_ref,
    send_sem, recv_sem, local_sem, result_sem, group_sem,
):
    t = pl.program_id(0)
    n = own_ref.shape[0]
    width = gw_ref.shape[-1]
    depth = part0_ref.shape[0]
    heads = width // HEAD_DIM
    step = n // 4
    place = Place()
    y = place.y
    links = Links(send_sem, recv_sem)
    k, i = group_and_block(t)
    mine = place.group(k)
    now = k % 2
    out = Result(links, place, own_ref, passing_ref, out_ref, step, result_sem.at[0], 4)
    layer = Result(links, place, layer_ref, passlayer_ref, layerout_ref, step, result_sem.at[1], 4)
    fetch = pltpu.make_async_copy(tokens_ref.at[place.t], own_ref, local_sem.at[0])
    fetch_layer, fetch_work, fetch_fold, fetch_gbt, fetch_a1t = [
        pltpu.make_async_copy(there, here, local_sem.at[1 + j])
        for j, (there, here) in enumerate([
            (layer_in, layer_ref), (work_in, work_ref), (fold_in, fold_ref),
            (gbt_in, gbt_ref), (a1t_in, a1t_ref),
        ])
    ]
    def operands(group):
        slot = group % 2
        pairs = [
            (gw_in, gw_ref), (scale_in, scale_ref), (o_in, o_ref), (v_in, v_ref),
            (q_in, q_ref), (kt_in, kt_ref), (gq_in, gq_ref),
        ]
        return [
            pltpu.make_async_copy(there.at[group], here.at[slot], group_sem.at[slot, j])
            for j, (there, here) in enumerate(pairs)
        ]

    corew = [links.add(place.to_core, stagew_ref, landw_ref.at[i]) for i in range(2)]
    core0 = [links.add(place.to_core, stage0_ref, land0_ref.at[i]) for i in range(2)]
    def half_done(i, *landing):
        return Reduce(
            links, place, lambda s, z, y: work_ref.at[i, z, y],
            lambda s, z: folded_ref.at[i, z] if s else fold_ref.at[i, z],
            *landing, slots=(1,),
        )

    seg1 = half_done(0, cross1_ref, far1_ref, mid1_ref, last1_ref, side1_ref)
    seg2 = half_done(1, cross2_ref, far2_ref, mid2_ref, last2_ref, side2_ref)
    segw = Reduce(
        links, place, lambda s, z, y: workw_ref.at[s, z, y],
        lambda s, z: workw_ref.at[s, z, y],
        crossw_ref, farw_ref, midw_ref, lastw_ref, sidew_ref,
    )
    seg0 = Reduce(
        links, place, lambda s, z, y: work0_ref.at[s, z, y],
        lambda s, z: work0_ref.at[s, z, y],
        cross0_ref, far0_ref, mid0_ref, last0_ref, side0_ref,
    )
    sum_core, sum_y, *sum_z, sum_x = [
        links.add(to, sums_ref.at[i], sumland_ref.at[j])
        for j, (i, to) in enumerate(
            zip([0, 1, 2, 2, 2, 3], [place.to_core, place.to_y] + place.to_z[1:] + [place.to_x])
        )
    ]

    def when(point):
        return pl.when(t == point)

    @when(0)
    def _():
        start(fetch_layer, operands(1), fetch_work, fetch_fold, fetch_gbt, operands(0))
        start(fetch, fetch_a1t)
        place.greet()
        fetch_layer.wait()
        for i in range(4):
            layer.send(i)
        fetch_work.wait()
        start(seg1.y[1], seg2.y[1])
        fetch_fold.wait()
        start(seg1.z[0][:2], seg2.z[0][:2])
        bqv_ref[...] = jnp.zeros_like(bqv_ref)
        sums_ref[0] = early_ref[...]
        fetch_gbt.wait()

    def add_core():
        recv(corew[1])

        @pl.loop(0, Z_DEV)
        def _(z):
            workw_ref[1, z] = (
                workw_ref[1, z].astype(F32) + landw_ref[1, z].astype(F32)
            ).astype(BF16)

        start(segw.y[1])

    def wait(copies):
        for copy in copies:
            copy.wait()

    @when(0)
    def _():
        wait(operands(1))

    @when(4)
    def _():
        start(operands(3))
        wait(operands(0))

    @when(8)
    def _():
        start(operands(2))
        wait(operands(3))

    @when(9)
    def _():
        wait(operands(2))

    plan = [
        (2, 1, lambda: (seg1.fold_y(1, 0), seg1.fold_z(0))),
        (3, 1, lambda: layer.pass_on(0)),
        (4, 0, lambda: (seg1.fold_y(1, 1), seg2.fold_z(0))),
        (4, 1, lambda: layer.pass_on(1)),
        (5, 1, lambda: (seg1.fold_z(1), seg2.fold_y(1, 0))),
        (8, 0, lambda: (seg2.fold_y(1, 1), layer.pass_on(2))),
        (8, 1, lambda: (seg1.send_x(), segw.fold_y(0, 0), segw.fold_y(0, 1))),
        (9, 0, add_core),
        (9, 1, lambda: (seg2.fold_z(1), seg0.fold_y(0, 0), layer.pass_on(3))),
        (10, 1, lambda: segw.fold_z(0)),
        (11, 1, lambda: (seg2.send_x(), seg0.fold_y(0, 1))),
        (12, 1, lambda: (segw.fold_y(1, 0), segw.fold_y(1, 1))),
        (13, 1, lambda: (seg0.fold_z(0), out.pass_on(3))),
        (14, 1, lambda: segw.fold_z(1)),
    ]

    def serve(point):
        for at, where, act in plan:
            if where == point:
                pl.when(t == at)(lambda act=act: (act(), None)[1])

    @pl.when((t == 0) | (t == 4) | (t == 8) | (t == 9))
    def _():
        pick = (
            lax.broadcasted_iota(jnp.int32, (8, width), 1) // HEAD_DIM
            == lax.broadcasted_iota(jnp.int32, (8, width), 0)
        ).astype(BF16)

        @pl.loop(0, n // step)
        def _(i):
            rows = pl.ds(pl.multiple_of(i * step, step), step)
            columns = scale_ref[now, :, rows].T
            lane = lax.broadcasted_iota(jnp.int32, (step, width), 1)
            scale = columns[:, heads - 1 : heads]
            for h in reversed(range(heads - 1)):
                scale = jnp.where(lane < (h + 1) * HEAD_DIM, columns[:, h : h + 1], scale)
            do = (dot_nn(gb_ref[rows, :], gw_ref[now]) * scale).astype(BF16)
            do_ref[now, rows, :] = do
            product = do.astype(F32) * o_ref[now, rows, :].astype(F32)
            high = product.astype(BF16)
            low = (product - high.astype(F32)).astype(BF16)
            delta_ref[now, :, rows] = dot_nt(pick, high) + dot_nt(pick, low)

        value = dot_nn(gbt_ref[...], o_ref[now]).reshape(Z_DEV, Y_DEV, depth, width)
        for s in range(2):
            @when(8 * s)
            def _():
                if s:
                    corew[0].wait_send()
                stagew_ref[...] = value.astype(BF16)
                start(corew[s])

        @when(4)
        def _():
            recv(corew[0])
            workw_ref[0] = (value + landw_ref[0].astype(F32)).astype(BF16)
            start(segw.y[0])

        @when(9)
        def _():
            workw_ref[1] = value.astype(BF16)

    serve(0)

    for ii in reversed(range(4)):
        @pl.when(i == ii)
        def _():
            first, last = ii * step, (ii + 1) * step
            do = do_ref[now, first:last, :]
            q = q_ref[now, first:last, :]
            v = v_ref[now, :last, :]
            lane = lax.broadcasted_iota(jnp.int32, (1, width), 1)
            dk, dv, dq = None, None, []
            for h in range(heads):
                low, high = h * HEAD_DIM, (h + 1) * HEAD_DIM
                here = (lane >= low) & (lane < high)
                p = p_ref[0, h, 0, :last, :]
                dp = dot_nt(v, jnp.where(here, do, jnp.zeros((), BF16)))
                ds = p * (dp - delta_ref[now, h : h + 1, first:last]).astype(BF16)
                part = dot_nn(p, do)
                dv = part if dv is None else jnp.where(lane < low, dv, part)
                part = dot_nn(ds, q)
                dk = part if dk is None else jnp.where(lane < low, dk, part)
                dq.append(dot_nn(kt_ref[now, low:high, :last], ds))
            if ii == 3:
                dkv_ref[now, 0] = dk
                dkv_ref[now, 1] = dv
            else:
                dkv_ref[now, 0, :last, :] += dk
                dkv_ref[now, 1, :last, :] += dv
            dk = dkv_ref[now, 0, first:last, :].astype(BF16)
            dv = dkv_ref[now, 1, first:last, :].astype(BF16)
            dq = (jnp.concatenate(dq, 0) * HEAD_DIM ** -0.5).astype(BF16).T
            dqkv_ref[now, first:last, :width] = dq
            dqkv_ref[now, first:last, width : 2 * width] = dk
            dqkv_ref[now, first:last, 2 * width :] = dv
            bqv_ref[mine, 0:1, :] += jnp.sum(dq.astype(F32), 0, keepdims=True)
            bqv_ref[mine, 1:2, :] += jnp.sum(dv.astype(F32), 0, keepdims=True)

            @pl.when(t >= 8)
            def _():
                da1_ref[first:last, :] += dot_nt(dqkv_ref[now, first:last, :], gq_ref[now])

    serve(1)

    @pl.when((t == 3) | (t == 7) | (t > 13))
    def _():
        @when(3)
        def _():
            fetch.wait()
            fetch_a1t.wait()

        @when(3)
        def _():
            da1_ref[...] = dot_nt(dqkv_ref[now], gq_ref[now])

        @when(7)
        def _():
            da1_ref[...] += dot_nt(dqkv_ref[now], gq_ref[now])

        value = dot_nn(a1t_ref[...], dqkv_ref[now]).reshape(Z_DEV, Y_DEV, depth, 3 * width)
        for s in range(2):
            @when(3 + 11 * s)
            def _():
                if s:
                    core0[0].wait_send()
                stage0_ref[...] = value.astype(BF16)
                start(core0[s])

            @when(7 + 8 * s)
            def _():
                recv(core0[s])
                work0_ref[s] = (value + land0_ref[s].astype(F32)).astype(BF16)
                start(seg0.y[s])

    @pl.when((t > 8) & (t % 2 == 1))
    def _():
        rows = pl.ds(pl.multiple_of(i * step, step), step)
        xhat, r = norm_parts(own_ref[rows, :].astype(F32))
        da1 = da1_ref[rows, :]
        sums_ref[0, 0:1, :] += jnp.sum(da1 * xhat, 0, keepdims=True)
        sums_ref[0, 2:3, :] += jnp.sum(da1, 0, keepdims=True)
        dg = da1 * rows_ref[0:1, :]
        dv = r * (
            dg
            - jnp.mean(dg, -1, keepdims=True)
            - xhat * jnp.mean(dg * xhat, -1, keepdims=True)
        )
        own_ref[rows, :] = (dh1_ref[...] + dv).astype(BF16)
        for ii in range(4):
            @pl.when(i == ii)
            def _():
                out.send(ii)

    @when(15)
    def _():
        for s in range(4):
            sums_ref[0, 3:5, s * width : (s + 1) * width] = bqv_ref[s, 0:2, :]
        start(sum_core)
        segw.send_x()
        out.pass_on(2)
        recv(sum_core)
        sums_ref[1] = sums_ref[0] + sumland_ref[0]
        start(sum_y)
        seg0.fold_y(1, 0)
        out.pass_on(1)
        seg0.fold_y(1, 1)
        recv(sum_y)
        sums_ref[2] = sums_ref[1] + sumland_ref[1]
        start(sum_z)
        seg0.fold_z(1)
        recv(sum_z)
        sums_ref[3] = (sums_ref[2] + sumland_ref[2]) + (sumland_ref[3] + sumland_ref[4])
        start(sum_x)
        part1_ref[...] = seg1.total()
        part2_ref[...] = seg2.total()
        seg0.send_x()
        partw_ref[...] = segw.total()
        layer.finish()
        out.pass_on(0)
        recv(sum_x)
        total_ref[...] = sums_ref[3] + sumland_ref[5]
        part0_ref[...] = seg0.total()
        out.finish()
        links.sent(corew[0], core0[0])


def group_and_block(t):
    early = t < 8
    return (
        jnp.where(early, 1 - t // 4, 3 - t % 2),
        3 - jnp.where(early, t % 4, jnp.maximum(t - 8, 0) // 2),
    )


def run_fused_backward(
    tokens, gq, gw, rows, dh1, gb, gbt, q, v, kt, p, scale, o, a1t, layer, fold, work, early
):
    groups, n, _ = tokens.shape
    width = gw.shape[-1]
    heads = width // HEAD_DIM
    hidden = fold.shape[-1]
    depth = D // (Z_DEV * Y_DEV)
    step = n // 4

    p_spec = pl.BlockSpec(
        (1, heads, 1, n, step),
        lambda t: (group_and_block(t)[0], 0, group_and_block(t)[1], 0, 0),
    )

    copies = 2 * 12 + 4 + 2 * 15 + 2 * 11 + 6

    def landing(lanes):
        return [
            pltpu.VMEM((2, Z_DEV, depth, lanes), BF16),
            pltpu.VMEM((2, 3, depth, lanes), BF16), pltpu.VMEM((2, 2, depth, lanes), BF16),
            pltpu.VMEM((depth, lanes), BF16), pltpu.VMEM((depth, lanes), BF16),
        ]

    def working(lanes):
        block = (Z_DEV, Y_DEV, depth, lanes)
        return [pltpu.VMEM(block, BF16)] + [pltpu.VMEM((2,) + block, BF16)] * 2

    return pl.pallas_call(
        fused_backward,
        grid=(4 * groups,),
        in_specs=[
            ANY_WHOLE, ANY_WHOLE, ANY_WHOLE, VMEM_WHOLE,
            pl.BlockSpec((step, D), lambda t: (group_and_block(jnp.maximum(t, 8))[1], 0)),
            VMEM_WHOLE, ANY_WHOLE, ANY_WHOLE, ANY_WHOLE, ANY_WHOLE, p_spec,
            ANY_WHOLE, ANY_WHOLE, ANY_WHOLE, ANY_WHOLE, ANY_WHOLE, ANY_WHOLE, VMEM_WHOLE,
        ],
        out_specs=[ANY_WHOLE] * 2 + [VMEM_WHOLE] * 5,
        out_shape=[
            shaped(BF16, groups, n, D), shaped(BF16, groups, n, D),
            shaped(F32, depth, 3 * width),
            shaped(F32, depth, width), shaped(F32, depth, hidden),
            shaped(F32, depth, hidden), shaped(F32, 16, D),
        ],
        scratch_shapes=[
            pltpu.VMEM((2, D, 3 * width), BF16), pltpu.VMEM((2, D, width), BF16),
            pltpu.VMEM((2, n, width), BF16), pltpu.VMEM((2, n, width), BF16),
            pltpu.VMEM((2, width, n), BF16), pltpu.VMEM((2, 8, n), F32),
            pltpu.VMEM((2, n, width), BF16),
            pltpu.VMEM((D, n), BF16), pltpu.VMEM((D, n), BF16), pltpu.VMEM((n, D), BF16),
            pltpu.VMEM((2, Z_DEV, depth, hidden), BF16),
            pltpu.VMEM((2, Z_DEV, Y_DEV, depth, hidden), BF16),
            pltpu.VMEM((2, n, width), BF16),
            pltpu.VMEM((2, 8, n), F32), pltpu.VMEM((2, 2, n, width), F32),
            pltpu.VMEM((2, n, 3 * width), BF16), pltpu.VMEM((n, D), F32),
            pltpu.VMEM((n, D), BF16), pltpu.VMEM((n, D), BF16), pltpu.VMEM((n, D), BF16),
            pltpu.VMEM((groups, 8, width), F32),
        ]
        + landing(hidden)[:1] + landing(hidden) + landing(hidden)
        + working(width) + landing(width)
        + working(3 * width) + landing(3 * width)
        + [
            pltpu.VMEM((4, 16, D), F32), pltpu.VMEM((6, 16, D), F32),
            pltpu.SemaphoreType.DMA((copies,)), pltpu.SemaphoreType.DMA((copies,)),
            pltpu.SemaphoreType.DMA((6,)), pltpu.SemaphoreType.DMA((2, 2, 4)),
            pltpu.SemaphoreType.DMA((2, 7)),
        ],
        compiler_params=pltpu.CompilerParams(
            vmem_limit_bytes=VMEM_LIMIT, collective_id=2, has_side_effects=True
        ),
        name="fused_backward",
    )(tokens, gq, gw, rows, dh1, gb, gbt, q, v, kt, p, scale, o, a1t, layer, fold, work, early)


def place_gradients(
    tie_ref, sums_ref, part0_ref, partw_ref, part1_ref, part2_ref, near_out_ref,
    near_grad_ref, far_out_ref, far_grad_ref, gains_ref, bias_ref, in_ref, out_ref, expand_ref,
    project_ref, chosen_ref,
):
    t = pl.program_id(0)
    far_out_ref[...] = near_out_ref[...]
    far_grad_ref[...] = near_grad_ref[...]
    own = gains_ref.shape[-1]
    width = partw_ref.shape[-1]
    kinds = [tie_ref[0], tie_ref[1], tie_ref[2], tie_ref[3]]

    @pl.when(t == 0)
    def _():
        first = (lax.axis_index("dp") * 4 + lax.axis_index("tensor")) * own
        feature = lax.broadcasted_iota(jnp.int32, (D, 128), 0)
        lane = lax.broadcasted_iota(jnp.int32, (D, 128), 1)
        chosen = ((feature == first + lane) & (lane < own)).astype(F32)
        chosen_ref[...] = lax.dot_general(
            sums_ref[...], chosen, (((1,), (0,)), ((), ())),
            precision=lax.Precision.HIGHEST, preferred_element_type=F32,
        )
        row = lax.broadcasted_iota(jnp.int32, (NSRC, own), 0)
        for i, kind in enumerate([0, 0, 0, 1, 2, 3, 2, 2, 2, 2]):
            value = chosen_ref[2 + i : 3 + i, :own]
            bias_ref[i] = jnp.where(row == kinds[kind], value, 0.0)

    @pl.when(t < NSRC)
    def _():
        def here(kind, value):
            return jnp.where(kinds[kind] == t, value, jnp.zeros_like(value))

        gains_ref[0, 0:1] = here(0, chosen_ref[0:1, :own])
        gains_ref[0, 1:2] = here(2, chosen_ref[1:2, :own])
        for j in range(3):
            in_ref[0, j] = here(0, part0_ref[:, j * width : (j + 1) * width])
        out_ref[0] = here(1, partw_ref[...].T)
        expand_ref[0] = here(2, part1_ref[...])
        project_ref[0] = here(3, part2_ref[...])


def run_place_gradients(tie, sums, part0, partw, part1, part2, out, grad, like):
    slots, n, _ = grad.shape
    gains, biases, w_in, w_out, w_expand, w_project = [item.shape for item in like]
    shapes = [
        gains, (biases[1], biases[0], biases[2]), w_in, w_out, w_expand,
        (w_project[0], w_project[2], w_project[1]),
    ]

    def source(shape):
        return pl.BlockSpec(
            (1,) + shape[1:], lambda t: (jnp.minimum(t, NSRC - 1),) + (0,) * (len(shape) - 1)
        )

    out, grad, gains, biases, w_in, w_out, w_expand, w_project = pl.pallas_call(
        place_gradients,
        grid=(slots,),
        in_specs=[SMEM_WHOLE] + [VMEM_WHOLE] * 5 + [group(n, D), group(n, D)],
        out_specs=[group(n, D), group(n, D), source(shapes[0]), VMEM_WHOLE]
        + [source(shape) for shape in shapes[2:]],
        out_shape=[shaped(BF16, slots, n, D)] * 2 + [shaped(F32, *item) for item in shapes],
        scratch_shapes=[pltpu.VMEM((16, 128), F32)],
        compiler_params=pltpu.CompilerParams(vmem_limit_bytes=VMEM_LIMIT),
        name="place_gradients",
    )(tie, sums, part0, partw, part1, part2, out, grad)
    biases = biases.transpose(1, 0, 2)
    return out, grad, gains, biases, w_in, w_out, w_expand, w_project.transpose(0, 2, 1)


def plain_step(
    tokens, lengths, tie_map, norm_gains, bias_rows, attention_in, attention_out,
    expand_weight, project_weight, cotangent,
):
    slot_rows = tokens.shape[0] // lengths.shape[0]
    me = lax.axis_index("tensor")
    in_local = lax.dynamic_index_in_dim(attention_in, tie_map[0], 0, keepdims=False)
    out_local = lax.dynamic_index_in_dim(attention_out, tie_map[1], 0, keepdims=False)
    expand_local = lax.dynamic_index_in_dim(expand_weight, tie_map[2], 0, keepdims=False)
    project_local = lax.dynamic_index_in_dim(project_weight, tie_map[3], 0, keepdims=False)
    local0 = jnp.concatenate([in_local, out_local.T[None]], 0)
    row_kinds = jnp.array([0, 0, 0, 1, 2, 3] + [2] * (FF // D), dtype=jnp.int32)
    gain_kinds = jnp.array([0, 2], dtype=jnp.int32)
    gain_pick = norm_gains[tie_map[gain_kinds], jnp.arange(2)]
    bias_pick = bias_rows[tie_map[row_kinds], jnp.arange(row_kinds.shape[0])]
    vectors = jnp.concatenate([gain_pick, bias_pick], 0)
    x = lax.dynamic_slice_in_dim(tokens, me * slot_rows, slot_rows, 0)
    cot = lax.dynamic_slice_in_dim(cotangent, me * slot_rows, slot_rows, 0)
    length = lax.dynamic_slice_in_dim(lengths, me, 1, 0)
    rows = lax.all_gather(vectors, ("dp", "tensor"), axis=1, tiled=True).astype(F32)
    rows = jnp.concatenate([rows, jnp.zeros((4, D), F32)], 0)

    def gathered(piece, axis):
        piece = lax.all_gather(piece, "dp", axis=axis, tiled=True)
        return lax.all_gather(piece, "tensor", axis=0)

    g0 = gathered(local0, 1)
    g1 = gathered(expand_local, 0)
    g2 = gathered(project_local.T, 0)
    groups, width = g0.shape[0], g0.shape[-1]
    bqv = rows[3:5].reshape(2, groups, width).transpose(1, 0, 2)
    q, v, kt, p, o, a1t, h1, a2, a2t = run_attention_forward(length, x, g0, rows, bqv)
    out, d1, d2, dh1, gb, gbt, sums = run_feed_forward(length, cot, a2, a2t, h1, g1, g2, rows)
    d0, xg, sums_in, sums_qv = run_attention_backward(
        x, g0, rows, dh1, gb, gbt, q, v, kt, p, o, a1t
    )
    layer_out = lax.all_gather(out, "tensor", axis=0, tiled=True)
    tokens_grad = lax.all_gather(xg, "tensor", axis=0, tiled=True)

    def scattered(piece, axis):
        piece = lax.psum_scatter(piece, "tensor", scatter_dimension=0)
        return lax.psum_scatter(piece, "dp", scatter_dimension=axis, tiled=True).astype(F32)

    part0 = scattered(d0, 1)
    part1 = scattered(d1, 0)
    part2 = scattered(d2, 0)
    qv = sums_qv[:, :2].transpose(1, 0, 2).reshape(2, D)
    sums = jnp.concatenate(
        [sums_in[0:1], sums[1:2], sums_in[1:2], qv, sums[5:12]], 0
    )
    sums = lax.psum_scatter(sums, ("dp", "tensor"), scatter_dimension=1, tiled=True)
    return layer_out, tokens_grad, *placed(tie_map, sums, part0, part1, part2)


def fused_step(
    tokens, lengths, tie_map, norm_gains, bias_rows, attention_in, attention_out,
    expand_weight, project_weight, cotangent,
):
    slots = lengths.shape[0]
    tokens = tokens.reshape(slots, -1, D)
    cotangent = cotangent.reshape(slots, -1, D)
    gq, gw, g1, g2, rows, q, v, kt, p, scale, o, a1t, h1, a2, a2t = run_fused_forward(
        tie_map, lengths, tokens, norm_gains, bias_rows, attention_in, attention_out,
        expand_weight, project_weight,
    )
    layer, fold, work, dh1, gb, gbt, early = run_fused_feed_forward(
        lengths, cotangent, a2, a2t, h1, g1, g2, rows
    )
    grad, out, part0, partw, part1, part2, sums = run_fused_backward(
        tokens, gq, gw, rows, dh1, gb, gbt, q, v, kt, p, scale, o, a1t, layer, fold,
        work, early,
    )
    out, grad, *placed_grads = run_place_gradients(
        tie_map, sums, part0, partw, part1, part2, out, grad,
        (norm_gains, bias_rows, attention_in, attention_out, expand_weight, project_weight),
    )
    return out.reshape(-1, D), grad.reshape(-1, D), *placed_grads


def placed(tie_map, sums, part0, part1, part2):
    source = jnp.arange(NSRC, dtype=jnp.int32)

    def place(piece, which):
        pick = (source == tie_map[which]).reshape((NSRC,) + (1,) * piece.ndim)
        return jnp.where(pick, piece[None], 0.0)

    def place_rows(piece, kinds):
        pick = source[:, None] == tie_map[jnp.array(kinds, dtype=jnp.int32)][None, :]
        return jnp.where(pick[:, :, None], piece[None], 0.0)

    return (
        place_rows(sums[:2], [0, 2]),
        place_rows(sums[2:], [0, 0, 0, 1, 2, 3] + [2] * (FF // D)),
        place(part0[:3], 0),
        place(part0[3].T, 1),
        place(part1, 2),
        place(part2.T, 3),
    )


def solution(mesh):
    fused = mesh.shape["dp"] == Z_DEV * Y_DEV and mesh.shape["tensor"] == X_DEV * C_DEV
    return jax.shard_map(
        fused_step if fused else plain_step,
        mesh=mesh,
        in_specs=(
            P("dp", None),
            P("dp"),
            P(),
            P(None, None, ("dp", "tensor")),
            P(None, None, ("dp", "tensor")),
            P(None, None, "dp", "tensor"),
            P(None, "tensor", "dp"),
            P(None, "dp", "tensor"),
            P(None, "tensor", "dp"),
            P("dp", None),
        ),
        out_specs=(
            P("dp", None),
            P("dp", None),
            P(None, None, ("dp", "tensor")),
            P(None, None, ("dp", "tensor")),
            P(None, None, "dp", "tensor"),
            P(None, "tensor", "dp"),
            P(None, "dp", "tensor"),
            P(None, "tensor", "dp"),
        ),
        check_vma=False,
    )
```

```python
import jax
import jax.numpy as jnp
from jax import lax
from jax.experimental import pallas as pl
from jax.experimental.pallas import tpu as pltpu
from jax.sharding import PartitionSpec as P

D = 768
HEAD_DIM = 64
FF = 3072
NSRC = 4
EPS = 1e-05
MASKED = -1e30
F32 = jnp.float32
BF16 = jnp.bfloat16
VMEM_LIMIT = 60 * 1024 * 1024


def dot_nn(a, b):
    return lax.dot_general(a, b, (((1,), (0,)), ((), ())), preferred_element_type=F32)


def dot_nt(a, b):
    return lax.dot_general(a, b, (((1,), (1,)), ((), ())), preferred_element_type=F32)


def norm_parts(v):
    center = jnp.mean(v, -1, keepdims=True)
    centered = v - center
    r = lax.rsqrt(jnp.mean(centered * centered, -1, keepdims=True) + EPS)
    return centered * r, r


def head_mask(shape, h):
    lane = lax.broadcasted_iota(jnp.int32, shape, 1)
    return (lane >= h * HEAD_DIM) & (lane < (h + 1) * HEAD_DIM)


def blocks(total, size):
    return [slice(i * size, (i + 1) * size) for i in range(total // size)]


def attention_forward(
    len_ref, x_ref, g_ref, rows_ref, bqv_ref,
    q_ref, v_ref, kt_ref, p_ref, o_ref, a1t_ref, h1_ref, a2_ref, a2t_ref,
    a1_ref, k_ref, vt_ref, ot_ref, attn_ref,
):
    t = pl.program_id(0)
    n = x_ref.shape[0]
    width = g_ref.shape[-1]
    heads = width // HEAD_DIM
    step = 256
    length = len_ref[0]

    @pl.when(t == 0)
    def _():
        @pl.loop(0, n // step)
        def _(b):
            rows = pl.ds(pl.multiple_of(b * step, step), step)
            xhat, _ = norm_parts(x_ref[rows, :].astype(F32))
            a1 = xhat * rows_ref[0:1, :] + rows_ref[2:3, :]
            a1_ref[rows, :] = a1.astype(BF16)
            a1t_ref[:, rows] = a1.astype(BF16).T
            attn_ref[rows, :] = x_ref[rows, :].astype(F32) + rows_ref[5:6, :]

    @pl.loop(0, n // step)
    def _(b):
        rows = pl.ds(pl.multiple_of(b * step, step), step)
        a1 = a1_ref[rows, :]
        q = (dot_nn(a1, g_ref[0, 0]) + bqv_ref[0, 0:1, :]).astype(BF16)
        q_ref[0, rows, :] = q * jnp.asarray(HEAD_DIM ** -0.5, BF16)
        k = dot_nn(a1, g_ref[0, 1]).astype(BF16)
        k_ref[rows, :] = k
        kt_ref[0, :, rows] = k.T
        v = (dot_nn(a1, g_ref[0, 2]) + bqv_ref[0, 1:2, :]).astype(BF16)
        v_ref[0, rows, :] = v
        vt_ref[:, rows] = v.T

    for h in range(heads):
        k = k_ref[...]
        k = jnp.where(head_mask(k.shape, h), k, jnp.zeros_like(k))
        for b in range(n // step):
            first, last = b * step, (b + 1) * step
            q = q_ref[0, first:last, :]
            key = lax.broadcasted_iota(jnp.int32, (last, step), 0)
            query = lax.broadcasted_iota(jnp.int32, (step, step), 1) + first
            s = dot_nt(k[:last], q)
            near = jnp.where(
                (key[first:] <= query) & (key[first:] < length), s[first:], MASKED
            )
            if b:
                far = jnp.where(key[:first] < length, s[:first], MASKED)
                top = jnp.maximum(
                    jnp.max(far, 0, keepdims=True), jnp.max(near, 0, keepdims=True)
                )
                e_far = jnp.exp(far - top)
                e_near = jnp.exp(near - top)
                total = jnp.sum(e_far, 0, keepdims=True) + jnp.sum(e_near, 0, keepdims=True)
                scale = 1.0 / total
                p_ref[0, h, :first, first:last] = (e_far * scale).astype(BF16)
            else:
                top = jnp.max(near, 0, keepdims=True)
                e_near = jnp.exp(near - top)
                scale = 1.0 / jnp.sum(e_near, 0, keepdims=True)
            p_ref[0, h, first:last, first:last] = (e_near * scale).astype(BF16)
            ot_ref[h * HEAD_DIM : (h + 1) * HEAD_DIM, first:last] = dot_nn(
                vt_ref[h * HEAD_DIM : (h + 1) * HEAD_DIM, :last],
                p_ref[0, h, :last, first:last],
            ).astype(BF16)

    @pl.loop(0, n // step)
    def _(b):
        rows = pl.ds(pl.multiple_of(b * step, step), step)
        o = ot_ref[:, rows].T
        o_ref[0, rows, :] = o
        attn_ref[rows, :] += dot_nt(o, g_ref[0, 3])

    @pl.when(t == pl.num_programs(0) - 1)
    def _():
        @pl.loop(0, n // step)
        def _(b):
            rows = pl.ds(pl.multiple_of(b * step, step), step)
            h1 = attn_ref[rows, :]
            h1_ref[rows, :] = h1
            xhat, _ = norm_parts(h1)
            a2 = (xhat * rows_ref[1:2, :] + rows_ref[6:7, :]).astype(BF16)
            a2_ref[rows, :] = a2
            a2t_ref[:, rows] = a2.T


SQRT_2_PI = 0.7978845608028654


def feed_forward_both(
    len_ref, c_ref, a2_ref, a2t_ref, h1_ref, w1_ref, w2_ref, rows_ref,
    out_ref, d1_ref, d2_ref, dh1_ref, gb_ref, gbt_ref, sums_ref,
    gf_ref, gft_ref, feed_ref, da2_ref, h_ref, df_ref,
):
    t = pl.program_id(0)
    n = c_ref.shape[0]
    step = 256
    length = len_ref[0]

    @pl.when(t == 0)
    def _():
        sums_ref[...] = jnp.zeros_like(sums_ref)

        @pl.loop(0, n // step)
        def _(b):
            rows = pl.ds(pl.multiple_of(b * step, step), step)
            place = b * step + lax.broadcasted_iota(jnp.int32, (step, 1), 0)
            live = (place < length).astype(F32)
            g = (c_ref[rows, :].astype(F32) * live).astype(BF16)
            gf_ref[rows, :] = g
            gft_ref[:, rows] = g.T
            sums_ref[7:8, :] += jnp.sum(g.astype(F32), 0, keepdims=True)

    bias = rows_ref[pl.ds(8 + t, 1), :]

    @pl.loop(0, n // step)
    def _(b):
        rows = pl.ds(pl.multiple_of(b * step, step), step)
        f = dot_nn(a2_ref[rows, :], w1_ref[0]) + bias
        dh = dot_nn(gf_ref[rows, :], w2_ref[0])
        f2 = f * f
        th = jnp.tanh(f * (SQRT_2_PI + (SQRT_2_PI * 0.044715) * f2))
        half = 0.5 + 0.5 * th
        h = (f * half).astype(BF16)
        slope = half + f * (0.5 - 0.5 * th * th) * (
            SQRT_2_PI + (3 * SQRT_2_PI * 0.044715) * f2
        )
        df = (dh * slope).astype(BF16)
        h_ref[rows, :] = h
        df_ref[rows, :] = df
        sums_ref[pl.ds(8 + t, 1), :] += jnp.sum(df.astype(F32), 0, keepdims=True)
        feed = dot_nt(h, w2_ref[0])
        da2 = dot_nt(df, w1_ref[0])

        @pl.when(t == 0)
        def _():
            feed_ref[rows, :] = feed
            da2_ref[rows, :] = da2

        @pl.when(t > 0)
        def _():
            feed_ref[rows, :] += feed
            da2_ref[rows, :] += da2

    @pl.loop(0, D // step)
    def _(b):
        rows = pl.ds(pl.multiple_of(b * step, step), step)
        d1_ref[0, rows, :] = dot_nn(a2t_ref[rows, :], df_ref[...]).astype(BF16)
        d2_ref[0, rows, :] = dot_nn(gft_ref[rows, :], h_ref[...]).astype(BF16)

    @pl.when(t == pl.num_programs(0) - 1)
    def _():
        @pl.loop(0, n // step)
        def _(b):
            rows = pl.ds(pl.multiple_of(b * step, step), step)
            place = b * step + lax.broadcasted_iota(jnp.int32, (step, 1), 0)
            live = (place < length).astype(F32)
            h1 = h1_ref[rows, :]
            out_ref[rows, :] = (live * (h1 + (feed_ref[rows, :] + rows_ref[7:8, :]))).astype(BF16)
            xhat, r = norm_parts(h1)
            da2 = da2_ref[rows, :]
            sums_ref[1:2, :] += jnp.sum(da2 * xhat, 0, keepdims=True)
            sums_ref[6:7, :] += jnp.sum(da2, 0, keepdims=True)
            dg = da2 * rows_ref[1:2, :]
            dv = r * (
                dg
                - jnp.mean(dg, -1, keepdims=True)
                - xhat * jnp.mean(dg * xhat, -1, keepdims=True)
            )
            dh1 = live * c_ref[rows, :].astype(F32) + dv
            dh1_ref[rows, :] = dh1
            gb = dh1.astype(BF16)
            gb_ref[rows, :] = gb
            gbt_ref[:, rows] = gb.T
            sums_ref[5:6, :] += jnp.sum(gb.astype(F32), 0, keepdims=True)


def attention_backward(
    x_ref, g_ref, rows_ref, dh1_ref, gb_ref, gbt_ref, q_ref, v_ref, kt_ref, p_ref,
    o_ref, a1t_ref,
    d0_ref, xg_ref, sums_ref, bqv_ref,
    do_ref, delta_ref, dqt_ref, dq_ref, dk_ref, dv_ref, da1_ref,
):
    t = pl.program_id(0)
    n = x_ref.shape[0]
    width = g_ref.shape[-1]
    heads = width // HEAD_DIM
    step = 256
    pick = (
        lax.broadcasted_iota(jnp.int32, (16, width), 1) // HEAD_DIM
        == lax.broadcasted_iota(jnp.int32, (16, width), 0)
    ).astype(BF16)

    @pl.loop(0, n // step)
    def _(b):
        rows = pl.ds(pl.multiple_of(b * step, step), step)
        do = dot_nn(gb_ref[rows, :], g_ref[0, 3]).astype(BF16)
        do_ref[rows, :] = do
        prod = do.astype(F32) * o_ref[0, rows, :].astype(F32)
        high = prod.astype(BF16)
        low = (prod - high.astype(F32)).astype(BF16)
        delta_ref[:, rows] = dot_nt(pick, high) + dot_nt(pick, low)

    dqt_ref[...] = jnp.zeros_like(dqt_ref)
    for b in range(n // step):
        first, last = b * step, (b + 1) * step
        do = do_ref[first:, :]
        q = q_ref[0, first:, :]
        v = v_ref[0, first:last, :]
        dk, dv = None, None
        for h in range(heads):
            mine = head_mask((1, width), h)
            zero = jnp.zeros((), BF16)
            p = p_ref[0, h, first:last, first:]
            dp = dot_nt(jnp.where(mine, v, zero), do)
            ds = (p.astype(F32) * (dp - delta_ref[h : h + 1, first:])).astype(BF16)
            part = dot_nn(p, jnp.where(mine, do, zero))
            dv = part if dv is None else dv + part
            part = dot_nn(ds, jnp.where(mine, q, zero))
            dk = part if dk is None else dk + part
            head = slice(h * HEAD_DIM, (h + 1) * HEAD_DIM)
            dqt_ref[head, first:] += dot_nn(kt_ref[0, head, first:last], ds)
        dk_ref[first:last, :] = dk.astype(BF16)
        dv_ref[first:last, :] = dv.astype(BF16)

    @pl.when(t == 0)
    def _():
        da1_ref[...] = jnp.zeros_like(da1_ref)

    bqv_ref[...] = jnp.zeros_like(bqv_ref)

    @pl.loop(0, n // step)
    def _(b):
        rows = pl.ds(pl.multiple_of(b * step, step), step)
        dq = (dqt_ref[:, rows] * HEAD_DIM ** -0.5).astype(BF16).T
        dk = dk_ref[rows, :]
        dv = dv_ref[rows, :]
        dq_ref[rows, :] = dq
        bqv_ref[0, 0:1, :] += jnp.sum(dq.astype(F32), 0, keepdims=True)
        bqv_ref[0, 1:2, :] += jnp.sum(dv.astype(F32), 0, keepdims=True)
        da1_ref[rows, :] += (
            dot_nt(dq, g_ref[0, 0]) + dot_nt(dk, g_ref[0, 1]) + dot_nt(dv, g_ref[0, 2])
        )

    @pl.loop(0, D // step)
    def _(b):
        rows = pl.ds(pl.multiple_of(b * step, step), step)
        a1t = a1t_ref[rows, :]
        d0_ref[0, 0, rows, :] = dot_nn(a1t, dq_ref[...]).astype(BF16)
        d0_ref[0, 1, rows, :] = dot_nn(a1t, dk_ref[...]).astype(BF16)
        d0_ref[0, 2, rows, :] = dot_nn(a1t, dv_ref[...]).astype(BF16)
        d0_ref[0, 3, rows, :] = dot_nn(gbt_ref[rows, :], o_ref[0]).astype(BF16)

    @pl.when(t == pl.num_programs(0) - 1)
    def _():
        sums_ref[...] = jnp.zeros_like(sums_ref)

        @pl.loop(0, n // step)
        def _(b):
            rows = pl.ds(pl.multiple_of(b * step, step), step)
            xhat, r = norm_parts(x_ref[rows, :].astype(F32))
            da1 = da1_ref[rows, :]
            sums_ref[0:1, :] += jnp.sum(da1 * xhat, 0, keepdims=True)
            sums_ref[1:2, :] += jnp.sum(da1, 0, keepdims=True)
            dg = da1 * rows_ref[0:1, :]
            dv = r * (
                dg
                - jnp.mean(dg, -1, keepdims=True)
                - xhat * jnp.mean(dg * xhat, -1, keepdims=True)
            )
            xg_ref[rows, :] = (dh1_ref[rows, :] + dv).astype(BF16)


def whole(*shape):
    return pl.BlockSpec(shape, lambda t: (0,) * len(shape))


def group(*shape):
    return pl.BlockSpec((1,) + shape, lambda t: (t,) + (0,) * len(shape))


def shaped(dtype, *shape):
    return jax.ShapeDtypeStruct(shape, dtype)


SMEM_WHOLE = pl.BlockSpec(memory_space=pltpu.SMEM)


def run_attention_forward(length, x, g0, rows, bqv):
    n = x.shape[0]
    groups, _, _, width = g0.shape
    heads = width // HEAD_DIM
    return pl.pallas_call(
        attention_forward,
        grid=(groups,),
        in_specs=[SMEM_WHOLE, whole(n, D), group(4, D, width), whole(16, D), group(2, width)],
        out_specs=[
            group(n, width), group(n, width), group(width, n), group(heads, n, n),
            group(n, width), whole(D, n), whole(n, D), whole(n, D), whole(D, n),
        ],
        out_shape=[
            shaped(BF16, groups, n, width), shaped(BF16, groups, n, width),
            shaped(BF16, groups, width, n), shaped(BF16, groups, heads, n, n),
            shaped(BF16, groups, n, width), shaped(BF16, D, n), shaped(F32, n, D),
            shaped(BF16, n, D), shaped(BF16, D, n),
        ],
        scratch_shapes=[
            pltpu.VMEM((n, D), BF16), pltpu.VMEM((n, width), BF16),
            pltpu.VMEM((width, n), BF16), pltpu.VMEM((width, n), BF16),
            pltpu.VMEM((n, D), F32),
        ],
        compiler_params=pltpu.CompilerParams(vmem_limit_bytes=VMEM_LIMIT),
        name="attention_forward",
    )(length, x, g0, rows, bqv)


def run_feed_forward(length, cot, a2, a2t, h1, g1, g2, rows):
    n = cot.shape[0]
    groups, _, width = g1.shape
    return pl.pallas_call(
        feed_forward_both,
        grid=(groups,),
        in_specs=[
            SMEM_WHOLE, whole(n, D), whole(n, D), whole(D, n), whole(n, D),
            group(D, width), group(D, width), whole(16, D),
        ],
        out_specs=[
            whole(n, D), group(D, width), group(D, width), whole(n, D), whole(n, D),
            whole(D, n), whole(16, D),
        ],
        out_shape=[
            shaped(BF16, n, D), shaped(BF16, groups, D, width), shaped(BF16, groups, D, width),
            shaped(F32, n, D), shaped(BF16, n, D), shaped(BF16, D, n), shaped(F32, 16, D),
        ],
        scratch_shapes=[
            pltpu.VMEM((n, D), BF16), pltpu.VMEM((D, n), BF16), pltpu.VMEM((n, D), F32),
            pltpu.VMEM((n, D), F32), pltpu.VMEM((n, width), BF16), pltpu.VMEM((n, width), BF16),
        ],
        compiler_params=pltpu.CompilerParams(vmem_limit_bytes=VMEM_LIMIT),
        name="feed_forward_both",
    )(length, cot, a2, a2t, h1, g1, g2, rows)


def run_attention_backward(x, g0, rows, dh1, gb, gbt, q, v, kt, p, o, a1t):
    n = x.shape[0]
    groups, _, _, width = g0.shape
    heads = width // HEAD_DIM
    return pl.pallas_call(
        attention_backward,
        grid=(groups,),
        in_specs=[
            whole(n, D), group(4, D, width), whole(16, D), whole(n, D), whole(n, D),
            whole(D, n), group(n, width), group(n, width), group(width, n),
            group(heads, n, n), group(n, width), whole(D, n),
        ],
        out_specs=[group(4, D, width), whole(n, D), whole(8, D), group(8, width)],
        out_shape=[
            shaped(BF16, groups, 4, D, width), shaped(BF16, n, D), shaped(F32, 8, D),
            shaped(F32, groups, 8, width),
        ],
        scratch_shapes=[
            pltpu.VMEM((n, width), BF16), pltpu.VMEM((16, n), F32), pltpu.VMEM((width, n), F32),
            pltpu.VMEM((n, width), BF16), pltpu.VMEM((n, width), BF16),
            pltpu.VMEM((n, width), BF16), pltpu.VMEM((n, D), F32),
        ],
        compiler_params=pltpu.CompilerParams(vmem_limit_bytes=VMEM_LIMIT),
        name="attention_backward",
    )(x, g0, rows, dh1, gb, gbt, q, v, kt, p, o, a1t)


Z_DEV, Y_DEV, X_DEV, C_DEV = 4, 2, 2, 2


class Place:
    def __init__(self):
        dp, self.t = lax.axis_index("dp"), lax.axis_index("tensor")
        self.dp = dp
        self.z, self.y = dp // 2, dp % 2
        self.x, self.c = self.t // 2, self.t % 2
        self.other_y = 1 - self.y
        self.zs = [
            self.z,
            self.z + 1 - 2 * (self.z % 2),
            self.z + 2 - 4 * (self.z // 2),
            3 - self.z,
        ]
        self.ts = [
            self.t,
            self.t + 1 - 2 * (self.t % 2),
            self.t + 2 - 4 * (self.t // 2),
            3 - self.t,
        ]
        self.to_z = [dict(dp=z * 2 + self.y) for z in self.zs]
        self.to_y = dict(dp=self.z * 2 + self.other_y)
        self.to_x = dict(tensor=self.ts[2])
        self.same_t = self.to_z[1:] + [dict(dp=z * 2 + self.other_y) for z in self.zs]
        self.same_dp = [dict(tensor=t) for t in self.ts[1:]]
        self.to_core = dict(tensor=self.ts[1])

    def group(self, k):
        return lax.select(
            k == 0, self.ts[0],
            lax.select(k == 1, self.ts[1], lax.select(k == 2, self.ts[2], self.ts[3])),
        )

    def greet(self, others=None):
        barrier = pltpu.get_barrier_semaphore()
        others = others or self.to_z[1:] + [self.to_y, self.to_x, self.to_core]
        for device in others:
            pl.semaphore_signal(
                barrier, inc=1, device_id=device, device_id_type=pl.DeviceIdType.MESH
            )
        pl.semaphore_wait(barrier, len(others))


class Pieces:
    def __init__(self, whole, pieces):
        self.whole, self.pieces = whole, pieces

    def start(self):
        for piece in self.pieces:
            piece.start()

    def wait_recv(self):
        self.whole.wait_recv()

    def wait_send(self):
        self.whole.wait_send()


class Links:
    def __init__(self, send_sem, recv_sem):
        self.send_sem, self.recv_sem = send_sem, recv_sem
        self.copies = []

    def add(self, device, src, dst, parts=1, axis=0):
        number = len(self.copies)

        def make(src, dst):
            return pltpu.make_async_remote_copy(
                src_ref=src,
                dst_ref=dst,
                send_sem=self.send_sem.at[number],
                recv_sem=self.recv_sem.at[number],
                device_id=device,
                device_id_type=pl.DeviceIdType.MESH,
            )

        size = src.shape[axis] // parts
        cuts = [(slice(None),) * axis + (pl.ds(i * size, size),) for i in range(parts)]
        copy = Pieces(make(src, dst), [make(src.at[cut], dst.at[cut]) for cut in cuts])
        self.copies.append(copy)
        return copy

    def sent(self, *apart):
        for copy in self.copies:
            if all(copy is not other for other in apart):
                copy.wait_send()


def flat(copies):
    for item in copies:
        if isinstance(item, list):
            yield from flat(item)
        else:
            yield item


def start(*copies):
    for copy in flat(copies):
        copy.start()


def recv(*copies):
    for copy in flat(copies):
        copy.wait_recv()


class Gather:
    def __init__(self, links, place, own, full, order, single=True, last=True):
        every = slice(None)
        y, other = place.y, place.other_y

        def same(device, k, yy, to):
            return links.add(device, full(k, every, yy), full(to, every, yy), Z_DEV)

        def along_z(k, yy, block):
            here, passed = full(k, place.z, yy), full(k, place.zs[2], yy)
            return [
                links.add(place.to_z[1], block, here),
                links.add(place.to_z[2], block, here),
                links.add(place.to_z[1], passed, passed),
            ]

        if order != WHOLE:
            self.z = along_z(0, y, own)
        if order == X_Z_Y:
            self.first = [links.add(place.to_x, own, full(2, place.z, y), 2)]
            self.far = along_z(2, y, full(2, place.z, y))
            blocks = [(0, y), (2, y), (0, other), (2, other)]
        else:
            blocks = [(0, y), (0, other), (2, y), (2, other)]
        if order == Y_Z_X:
            self.first = [links.add(place.to_y, own, full(0, place.z, y), 2)]
            self.far = along_z(0, other, full(0, place.z, other))
        if order == Z_Y_X and single:
            self.first = [same(place.to_y, 0, y, 0)]
        if order == Z_Y_X and not single:
            self.first = [links.add(place.to_y, own, full(0, place.z, y))]
            for k in range(1, 4):
                block = full(0, place.zs[k], y)
                self.first.append(links.add(place.to_y, block, block))
            return
        self.second = [
            same(place.to_y, k, yy, k) if order == X_Z_Y else same(place.to_x, k, yy, 2)
            for k, yy in blocks[: 2 if last else 1]
        ]
        if not last:
            blocks = [block for block in blocks if block[0] == 0]
        self.core = [same(place.to_core, k, yy, k + 1) for k, yy in blocks]


Z_Y_X, Y_Z_X, X_Z_Y, WHOLE = range(4)


def fused_forward(
    tie_ref, len_ref, tokens_ref, gains_ref, bias_ref, in_ref, out_ref, expand_ref,
    project_ref,
    gq_ref, gw_ref, flat1_ref, flat2_ref, rows_ref,
    q_ref, v_ref, kt_ref, p_ref, scale_ref, o_ref, a1t_out, h1_out, a2_out, a2t_out,
    own0_ref, ownw_ref, own1_ref, own2_ref, square_ref, vec_ref,
    all0_ref, allw_ref, w1_ref, w2_ref, vecs_ref, bqv_ref, x_ref, a1_ref, k_ref, qa_ref, vt_ref, ot_ref, a1t_ref, h1_ref, a2_ref, a2t_ref,
    send_sem, recv_sem, local_sem, flush_sem, row_sem,
):
    t, h = pl.program_id(0), pl.program_id(1)
    n, _ = x_ref.shape
    width = allw_ref.shape[-1]
    heads = width // HEAD_DIM
    step = 256
    place = Place()
    length = len_ref[place.t]
    links = Links(send_sem, recv_sem)
    z, y, x, c = place.z, place.y, place.x, place.c
    mine_there = vecs_ref.at[z, y, x, c]
    column = vecs_ref.at[:, :, x, c]
    vec_one = [links.add(device, vec_ref, mine_there) for device in place.same_t]
    vec_two = [links.add(device, column, column) for device in place.same_dp]
    half = own0_ref.shape[0] // 2
    halves = []
    for i in range(2):
        rows = pl.ds(i * half, half)
        halves.append(Gather(
            links, place, own0_ref.at[rows],
            lambda k, z, y, rows=rows: all0_ref.at[k, z, y, rows], Z_Y_X, single=False,
        ))
    seg0 = Gather(links, place, own0_ref, lambda k, z, y: all0_ref.at[k, z, y], WHOLE)
    segw = Gather(links, place, ownw_ref, lambda k, z, y: allw_ref.at[k, z, y], Z_Y_X)
    seg1 = Gather(
        links, place, own1_ref, lambda k, z, y: w1_ref.at[k, z, y], Z_Y_X, last=False
    )
    seg2 = Gather(
        links, place, own2_ref, lambda k, z, y: w2_ref.at[k, z, y], X_Z_Y, last=False
    )
    flush = [
        [
            pltpu.make_async_copy(ref.at[k], flat.at[k], flush_sem.at[i, k])
            for k in range(3)
        ]
        for i, (ref, flat) in enumerate([(w1_ref, flat1_ref), (w2_ref, flat2_ref)])
    ]
    put_a1t = pltpu.make_async_copy(a1t_ref, a1t_out, local_sem.at[0])
    put_a2t = pltpu.make_async_copy(a2t_ref, a2t_out, local_sem.at[1])
    puts = []
    for i in range(n // step):
        rows = pl.ds(i * step, step)
        puts.append([
            pltpu.make_async_copy(h1_ref.at[rows], h1_out.at[rows], row_sem.at[0, i]),
            pltpu.make_async_copy(a2_ref.at[rows], a2_out.at[rows], row_sem.at[1, i]),
        ])
    fetch = pltpu.make_async_copy(tokens_ref.at[place.t], x_ref, local_sem.at[2])

    def relay_z(copies):
        recv(copies[1])
        start(copies[2])

    def pass_own(seg):
        recv(seg.z[0], seg.z[2])
        if seg is not seg2:
            start(seg.first)
        start(seg.second[0], seg.core[0])

    def pass_second(seg):
        recv(seg.second)
        if seg is seg2:
            start(seg.core[1])

    def pass_first(seg):
        recv(seg.first)
        if seg is segw:
            start(seg.second[1], seg.core[1])
        elif seg is seg1:
            start(seg.core[1])
        else:
            start(seg.far[1], seg.far[0])

    def pass_far(seg):
        recv(seg.far[0], seg.far[2])

    def pass_core(seg, i):
        recv(seg.second[i])
        start(seg.core[2 + i])

    plan = [
        (0, 0, lambda: (pass_own(segw), relay_z(seg2.z), pass_first(seg2))),
        (0, 2, lambda: relay_z(seg1.z)),
        (0, 3, lambda: (pass_first(segw), pass_core(seg0, 0))),
        (1, 0, lambda: recv(seg0.core[:2])),
        (1, 1, lambda: pass_own(seg1)),
        (1, 2, lambda: relay_z(seg2.far)),
        (1, 3, lambda: pass_core(seg0, 1)),
        (1, 4, lambda: (recv(segw.core[:2]), pass_core(segw, 0), pass_own(seg2))),
        (2, 2, lambda: pass_core(segw, 1)),
        (2, 4, lambda: (pass_first(seg1), flush[0][0].start())),
        (3, 0, lambda: recv(seg0.core[2:])),
        (3, 2, lambda: (pass_second(seg2), flush[1][0].start())),
        (3, 3, lambda: (pass_far(seg2), flush[1][2].start())),
        (3, 4, lambda: recv(segw.core[2:])),
    ]

    def serve(points):
        for step, where, act in plan:
            if where in points:
                now = (t == step) & (h == max(where - 2, 0))
                pl.when(now)(lambda act=act: (act(), None)[1])

    @pl.when((t == 0) & (h == 0))
    def _():
        s0, s1, s2, s3 = tie_ref[0], tie_ref[1], tie_ref[2], tie_ref[3]
        fetch.start()
        square_ref[...] = jnp.zeros_like(square_ref)
        gain = gains_ref.shape[-1]
        square_ref[0:1, :gain] = gains_ref[s0].astype(F32)[0:1]
        square_ref[1:2, :gain] = gains_ref[s2].astype(F32)[1:2]
        kinds = [s0, s0, s0, s1, s2, s3, s2, s2, s2, s2]
        for i, source in enumerate(kinds):
            wide = bias_ref[i].astype(F32)
            here = lax.broadcasted_iota(jnp.int32, wide.shape, 0) == source
            square_ref[2 + i : 3 + i, :gain] = jnp.sum(
                jnp.where(here, wide, 0.0), 0, keepdims=True
            )
        vec_ref[...] = square_ref[...].T[:gain]
        for j in range(3):
            own0_ref[:, j * width : (j + 1) * width] = in_ref[s0, j]
        place.greet(place.same_t + place.same_dp)
        start(vec_one)
        for part in halves:
            start(part.z[1], part.z[0], part.first[0])
        vecs_ref[z, y, x, c] = vec_ref[...]
        ones = lax.broadcasted_iota(jnp.int32, (vt_ref.shape[1] - HEAD_DIM, n), 0) == 0
        for h in range(heads):
            vt_ref[h, HEAD_DIM:, :] = ones.astype(BF16)
        all0_ref[0, z, y] = own0_ref[...]
        ownw_ref[...] = out_ref[s1].T
        allw_ref[0, z, y] = ownw_ref[...]
        own1_ref[...] = expand_ref[s2]
        own2_ref[...] = project_ref[s3]
        w1_ref[0, z, y] = own1_ref[...]
        w2_ref[0, z, y] = own2_ref[...]
        recv(vec_one)
        start(vec_two)
        for part in halves:
            relay_z(part.z)
            start(part.first[2])
        for part in halves:
            recv(part.z[0])
            start(part.first[1])
        start(segw.z[1], segw.z[0], seg2.z[1])
        recv(vec_two)
        start(seg2.first)
        vecs = vecs_ref[...].reshape(D, vecs_ref.shape[-1]).T[:16]
        rows_ref[...] = vecs
        for part in halves:
            recv(part.z[2])
            start(part.first[3])
        start(seg0.second[0], seg0.core[0])
        for k in range(4):
            part = slice(k * width, (k + 1) * width)
            bqv_ref[k, 0:1, :width] = vecs[3:4, part]
            bqv_ref[k, 0:1, width : 2 * width] = jnp.zeros((1, width), F32)
            bqv_ref[k, 0:1, 2 * width :] = vecs[4:5, part]
        fetch.wait()

        @pl.loop(0, n // step)
        def _(b):
            rows = pl.ds(pl.multiple_of(b * step, step), step)
            wide = x_ref[rows, :].astype(F32)
            xhat, _ = norm_parts(wide)
            a1 = (xhat * rows_ref[0:1, :] + rows_ref[2:3, :]).astype(BF16)
            a1_ref[rows, :] = a1
            a1t_ref[:, rows] = a1.T
            h1_ref[rows, :] = wide + rows_ref[5:6, :]

        put_a1t.start()
        relay_z(segw.z)
        start(seg2.z[0], seg1.z[1], seg1.z[0])
        recv(halves[0].first, halves[1].first)
        start(seg0.second[1], seg0.core[1])

    serve([0])

    @pl.when(h == 0)
    def _():
        gq = all0_ref[t].reshape(D, 3 * width)
        gq_ref[0] = gq
        mine = place.group(t)
        qkv = dot_nn(a1_ref[...], gq) + bqv_ref[mine, 0:1, :]
        q = qkv[:, :width].astype(BF16) * jnp.asarray(HEAD_DIM ** -0.5, BF16)
        k = qkv[:, width : 2 * width].astype(BF16)
        v = qkv[:, 2 * width :].astype(BF16)
        q_ref[0] = q
        kt_ref[0] = k.T
        v_ref[0] = v
        vt = v.T
        for h in range(heads):
            vt_ref[h, :HEAD_DIM, :] = vt[h * HEAD_DIM : (h + 1) * HEAD_DIM]
        spare = k_ref.shape[1] - width
        dead = lax.broadcasted_iota(jnp.int32, (n, spare), 0) >= length
        first_column = lax.broadcasted_iota(jnp.int32, (n, spare), 1) == 0
        k_ref[:, :width] = k
        k_ref[:, width:] = jnp.where(first_column & dead, MASKED, 0.0).astype(BF16)
        qa_ref[:, :width] = q
        qa_ref[:, width:] = jnp.where(first_column, 1.0, 0.0).astype(BF16)
        scale_ref[0, heads:, :] = jnp.zeros((scale_ref.shape[1] - heads, n), F32)

    serve([1])

    lane = lax.broadcasted_iota(jnp.int32, (1, qa_ref.shape[1]), 1)
    keep = ((lane >= h * HEAD_DIM) & (lane < (h + 1) * HEAD_DIM)) | (lane >= width)
    key = lax.broadcasted_iota(jnp.int32, (step, step), 0)
    query = lax.broadcasted_iota(jnp.int32, (step, step), 1)
    head = pl.ds(pl.multiple_of(h * HEAD_DIM, HEAD_DIM), HEAD_DIM)

    def scores(b):
        first, last = b * step, (b + 1) * step
        q = jnp.where(keep, qa_ref[first:last, :], jnp.zeros((), BF16))
        return dot_nt(k_ref[:last, :], q)

    def attend(b, s):
        first, last = b * step, (b + 1) * step
        near = jnp.where(key <= query, s[first:], MASKED)
        top = jnp.max(near, 0, keepdims=True)
        if b:
            far = s[:first]
            top = jnp.maximum(top, jnp.max(far, 0, keepdims=True))
        e_near = jnp.exp((near - top).astype(BF16))
        p_ref[0, 0, b, first:last, :] = e_near
        o = dot_nn(vt_ref[h, :, first:last], e_near)
        if b:
            e_far = jnp.exp((far - top).astype(BF16))
            p_ref[0, 0, b, :first, :] = e_far
            o += dot_nn(vt_ref[h, :, :first], e_far)
        scale = 1.0 / o[HEAD_DIM : HEAD_DIM + 1]
        scale_ref[0, pl.ds(h, 1), first:last] = scale
        ot_ref[head, first:last] = (o[:HEAD_DIM] * scale).astype(BF16)

    s = scores(0)
    for b in range(n // step):
        ahead = scores(b + 1) if b + 1 < n // step else None
        attend(b, s)
        s = ahead

    serve([2, 3, 4])

    @pl.when(h == heads - 1)
    def _():
        gw_ref[0] = allw_ref[t].reshape(gw_ref.shape[1:])
        o = ot_ref[...].T
        o_ref[0] = o
        h1_ref[...] += dot_nt(o, gw_ref[0])

    @pl.when((t == 3) & (h == heads - 1))
    def _():
        for i, rows in enumerate(blocks(n, step)):
            xhat, _ = norm_parts(h1_ref[rows, :])
            a2 = (xhat * rows_ref[1:2, :] + rows_ref[6:7, :]).astype(BF16)
            a2_ref[rows, :] = a2
            a2t_ref[:, rows] = a2.T
            for put in puts[i]:
                put.start()
        put_a2t.start()
        recv(seg2.core)
        flush[1][1].start()
        recv(seg1.core)
        flush[0][1].start()
        pass_second(seg1)
        flush[0][2].start()
        links.sent()
        for copies in flush + puts + [[put_a1t, put_a2t]]:
            for copy in copies:
                copy.wait()


N_GATHER = 10 + 14 + 6 + 10 + 7 + 10
VMEM_WHOLE = pl.BlockSpec(memory_space=pltpu.VMEM)
ANY_WHOLE = pl.BlockSpec(memory_space=pl.ANY)


def run_fused_forward(tie, lengths, tokens, gains, biases, w_in, w_out, w_expand, w_project):
    groups, n, _ = tokens.shape
    depth, width = w_in.shape[-2:]
    heads = width // HEAD_DIM
    hidden = w_expand.shape[-1]
    w_project = w_project.transpose(0, 2, 1)
    biases = biases.transpose(1, 0, 2)
    own = gains.shape[-1]

    def group(*shape):
        return pl.BlockSpec((1,) + shape, lambda t, h: (t,) + (0,) * len(shape))

    per_head = pl.BlockSpec((1, 1, n // 256, n, 256), lambda t, h: (t, h, 0, 0, 0))
    return pl.pallas_call(
        fused_forward,
        grid=(groups, heads),
        in_specs=[SMEM_WHOLE, SMEM_WHOLE, ANY_WHOLE] + [VMEM_WHOLE] * 6,
        out_specs=[
            group(D, 3 * width), group(D, width), ANY_WHOLE, ANY_WHOLE, VMEM_WHOLE,
            group(n, width), group(n, width), group(width, n), per_head,
            group(8, n), group(n, width), ANY_WHOLE, ANY_WHOLE, ANY_WHOLE, ANY_WHOLE,
        ],
        out_shape=[
            shaped(BF16, groups, D, 3 * width), shaped(BF16, groups, D, width),
            shaped(BF16, groups, Z_DEV, Y_DEV, depth, hidden),
            shaped(BF16, groups, Z_DEV, Y_DEV, depth, hidden),
            shaped(F32, 16, D),
            shaped(BF16, groups, n, width), shaped(BF16, groups, n, width),
            shaped(BF16, groups, width, n), shaped(BF16, groups, heads, n // 256, n, 256),
            shaped(F32, groups, 8, n), shaped(BF16, groups, n, width), shaped(BF16, D, n), shaped(F32, n, D),
            shaped(BF16, n, D), shaped(BF16, D, n),
        ],
        scratch_shapes=[
            pltpu.VMEM((depth, 3 * width), BF16), pltpu.VMEM((depth, width), BF16),
            pltpu.VMEM((depth, hidden), BF16), pltpu.VMEM((depth, hidden), BF16),
            pltpu.VMEM((128, 128), F32), pltpu.VMEM((own, 128), F32),
            pltpu.VMEM((groups, Z_DEV, Y_DEV, depth, 3 * width), BF16),
            pltpu.VMEM((groups, Z_DEV, Y_DEV, depth, width), BF16),
            pltpu.VMEM((groups, Z_DEV, Y_DEV, depth, hidden), BF16),
            pltpu.VMEM((groups, Z_DEV, Y_DEV, depth, hidden), BF16),
            pltpu.VMEM((Z_DEV, Y_DEV, X_DEV, C_DEV, own, 128), F32),
            pltpu.VMEM((groups, 8, 3 * width), F32),
            pltpu.VMEM((n, D), BF16), pltpu.VMEM((n, D), BF16), pltpu.VMEM((n, 256), BF16),
            pltpu.VMEM((n, 256), BF16), pltpu.VMEM((heads, HEAD_DIM + 16, n), BF16),
            pltpu.VMEM((width, n), BF16),
            pltpu.VMEM((D, n), BF16), pltpu.VMEM((n, D), F32), pltpu.VMEM((n, D), BF16),
            pltpu.VMEM((D, n), BF16),
            pltpu.SemaphoreType.DMA((N_GATHER,)), pltpu.SemaphoreType.DMA((N_GATHER,)),
            pltpu.SemaphoreType.DMA((3,)), pltpu.SemaphoreType.DMA((2, 4)),
            pltpu.SemaphoreType.DMA((2, n // 256)),
        ],
        compiler_params=pltpu.CompilerParams(
            vmem_limit_bytes=VMEM_LIMIT, collective_id=0, has_side_effects=True
        ),
        name="fused_forward",
    )(tie, lengths, tokens, gains, biases, w_in, w_out, w_expand, w_project)


class Result:
    def __init__(self, links, place, own_ref, passing_ref, out_ref, step, sem, count):
        self.x, self.core, self.far, self.keep, self.keep_far = [], [], [], [], []
        for i in range(count):
            rows = pl.ds(i * step, step)
            mine, theirs = out_ref.at[place.t, rows], out_ref.at[place.ts[2], rows]
            own, passing = own_ref.at[rows], passing_ref.at[rows]
            self.x.append(links.add(place.to_x, own, passing))
            self.core.append(links.add(place.to_core, own, mine))
            self.far.append(links.add(place.to_core, passing, theirs))
            self.keep.append(pltpu.make_async_copy(own, mine, sem.at[0, i]))
            self.keep_far.append(pltpu.make_async_copy(passing, theirs, sem.at[1, i]))

    def send(self, i):
        start(self.x[i], self.core[i], self.keep[i])

    def pass_on(self, i):
        recv(self.x[i])
        start(self.far[i], self.keep_far[i])

    def finish(self):
        recv(self.core, self.far)
        for copy in self.keep + self.keep_far:
            copy.wait()


def low(value):
    return jnp.asarray(value, BF16)


def pair_order(i):
    return i + 1 - 2 * (i % 2)


def fused_feed_forward(
    len_ref, cot_ref, a2_ref, a2t_in, h1_in, far1_ref, far2_ref, rows_ref,
    out_out, fold_ref, work_out, dh1_out, gb_out, gbt_out, sums_ref,
    gf_ref, gft_ref, feed_ref, da2_ref, h_ref, df_ref, weights_ref, missing_ref, third_ref,
    stage_ref, land_ref, near_ref, cross_ref, a2t_ref, h1_ref, out_ref, work_ref,
    send_sem, recv_sem, local_sem, row_sem,
):
    t = pl.program_id(0)
    n = gf_ref.shape[0]
    step = 256
    depth = stage_ref.shape[-2]
    place = Place()
    length = len_ref[place.t]
    links = Links(send_sem, recv_sem)
    y, other = place.y, place.other_y
    last = [
        links.add(place.to_x, far1_ref.at[0, :, other], missing_ref.at[0, 0]),
        links.add(place.to_y, far2_ref.at[2, :, y], missing_ref.at[1, 0]),
    ]
    last_core = [
        links.add(place.to_core, missing_ref.at[i, 0], missing_ref.at[i, 1]) for i in range(2)
    ]
    third = [
        links.add(place.to_core, far_ref.at[2, :, y], third_ref.at[i])
        for i, far_ref in enumerate([far1_ref, far2_ref])
    ]
    core = [
        [links.add(place.to_core, stage_ref.at[i], land_ref.at[s, i]) for i in range(2)]
        for s in range(2)
    ]
    cross = [
        links.add(place.to_y, near_ref.at[i, :, other], cross_ref.at[i]) for i in range(2)
    ]
    fetch = pltpu.make_async_copy(cot_ref.at[place.t], gf_ref, local_sem.at[0])
    gb_ref, gbt_ref, dh1_ref = gf_ref, gft_ref, da2_ref
    late = [
        pltpu.make_async_copy(a2t_in, a2t_ref, local_sem.at[5]),
        pltpu.make_async_copy(h1_in, h1_ref, local_sem.at[6]),
    ]
    puts = []
    for i in range(n // step):
        rows = pl.ds(i * step, step)
        puts.append([
            pltpu.make_async_copy(ref.at[rows], out.at[rows], row_sem.at[j, i])
            for j, (ref, out) in enumerate(
                [(out_ref, out_out), (dh1_ref, dh1_out), (gb_ref, gb_out)]
            )
        ])
    put_gbt = pltpu.make_async_copy(gbt_ref, gbt_out, local_sem.at[7])
    put_work = pltpu.make_async_copy(work_ref, work_out, local_sem.at[8])
    k = pair_order(t)
    mine = place.group(k)

    def load(step, whole, slot):
        for i, far_ref in enumerate([far1_ref, far2_ref]):
            group = far_ref.at[pair_order(step)]
            to = weights_ref.at[slot, i]
            if not whole:
                group, to = group.at[:, y], to.at[:, y]
            yield pltpu.make_async_copy(group, to, local_sem.at[1 + 2 * slot + i])

    def live_rows(b):
        at = b * step + lax.broadcasted_iota(jnp.int32, (step, 1), 0)
        return (at < length).astype(F32)

    @pl.when(t == 0)
    def _():
        fetch.start()
        for copy in load(0, True, 0):
            copy.start()
        for copy in late:
            copy.start()
        place.greet()
        start(last, third)
        sums_ref[...] = jnp.zeros_like(sums_ref)
        feed_ref[...] = jnp.zeros_like(feed_ref)
        da2_ref[...] = jnp.zeros_like(da2_ref)
        fetch.wait()

        @pl.loop(0, n // step)
        def _(b):
            rows = pl.ds(pl.multiple_of(b * step, step), step)
            g = (gf_ref[rows, :].astype(F32) * live_rows(b)).astype(BF16)
            gf_ref[rows, :] = g
            gft_ref[:, rows] = g.T
            sums_ref[7:8, :] += jnp.sum(g.astype(F32), 0, keepdims=True)

    for i in range(4):
        @pl.when(t == i)
        def _():
            if i == 2:
                recv(last_core, third)
            else:
                for copy in load(i, i < 2, i % 2):
                    copy.wait()
            if i in (0, 2):
                for copy in load(i + 1, i + 1 < 2, (i + 1) % 2):
                    copy.start()
            for j in range(2):
                if i == 2:
                    weights_ref[0, j, :, y] = third_ref[j]
                if i >= 2:
                    weights_ref[i % 2, j, :, other] = missing_ref[j, 3 - i]

    bias = rows_ref[pl.ds(8 + mine, 1), :]
    w1 = weights_ref[t % 2, 0].reshape(D, -1)
    w2 = weights_ref[t % 2, 1].reshape(D, -1)
    column = jnp.zeros((1, w1.shape[1]), F32)
    for rows in blocks(n, step):
        f = (dot_nn(a2_ref[rows, :], w1) + bias).astype(BF16)
        dh = dot_nn(gf_ref[rows, :], w2)
        f2 = f * f
        th = jnp.tanh(f * (low(SQRT_2_PI) + low(SQRT_2_PI * 0.044715) * f2))
        half = low(0.5) + low(0.5) * th
        h = f * half
        slope = half + f * (low(0.5) - low(0.5) * th * th) * (
            low(SQRT_2_PI) + low(3 * SQRT_2_PI * 0.044715) * f2
        )
        df = (dh * slope.astype(F32)).astype(BF16)
        h_ref[rows, :] = h
        df_ref[rows, :] = df
        column += jnp.sum(df.astype(F32), 0, keepdims=True)
        feed_ref[rows, :] += dot_nt(h, w2)
        da2_ref[rows, :] += dot_nt(df, w1)
    sums_ref[pl.ds(8 + mine, 1), :] = column

    @pl.when(t == 1)
    def _():
        recv(last)
        start(last_core)

    @pl.when(t == 0)
    def _():
        late[0].wait()

    def weight_grad(left_ref, right_ref):
        value = dot_nn(left_ref[...], right_ref[...])
        return value.reshape(Z_DEV, Y_DEV, depth, value.shape[-1]).astype(BF16)

    grad1 = weight_grad(a2t_ref, df_ref)
    grad2 = weight_grad(gft_ref, h_ref)

    def put(ref):
        ref[0] = grad1
        ref[1] = grad2

    def reduced(ref):
        return lambda i, s, z: (
            ref[i, z].astype(F32) + land_ref[s, i, z].astype(F32)
        ).astype(BF16)

    @pl.when(t == 0)
    def _():
        put(stage_ref)
        start(core[0])

    @pl.when(t == 1)
    def _():
        put(near_ref)
        recv(core[0])

        @pl.loop(0, Z_DEV)
        def _(z):
            for i in range(2):
                near_ref[i, z] = reduced(near_ref)(i, 0, z)

        start(cross)

    @pl.when(t == 2)
    def _():
        for copy in core[0]:
            copy.wait_send()
        put(stage_ref)
        start(core[1])

    @pl.when(t == 3)
    def _():
        put(work_ref)
        late[1].wait()
        for i, rows in enumerate(blocks(n, step)):
            live = live_rows(i)
            h1 = h1_ref[rows, :]
            out_ref[rows, :] = (live * (h1 + (feed_ref[rows, :] + rows_ref[7:8, :]))).astype(BF16)
            xhat, r = norm_parts(h1)
            da2 = da2_ref[rows, :]
            sums_ref[1:2, :] += jnp.sum(da2 * xhat, 0, keepdims=True)
            sums_ref[6:7, :] += jnp.sum(da2, 0, keepdims=True)
            dg = da2 * rows_ref[1:2, :]
            dv = r * (
                dg
                - jnp.mean(dg, -1, keepdims=True)
                - xhat * jnp.mean(dg * xhat, -1, keepdims=True)
            )
            dh1 = gf_ref[rows, :].astype(F32) + dv
            dh1_ref[rows, :] = dh1
            gb = dh1.astype(BF16)
            gb_ref[rows, :] = gb
            gbt_ref[:, rows] = gb.T
            sums_ref[5:6, :] += jnp.sum(gb.astype(F32), 0, keepdims=True)
            for copy in puts[i]:
                copy.start()
        put_gbt.start()
        recv(core[1])

        @pl.loop(0, Z_DEV)
        def _(z):
            for i in range(2):
                work_ref[i, z] = reduced(work_ref)(i, 1, z)

        put_work.start()
        recv(cross)

        @pl.loop(0, Z_DEV)
        def _(z):
            for i in range(2):
                fold_ref[i, z] = (
                    near_ref[i, z, y].astype(F32) + cross_ref[i, z].astype(F32)
                ).astype(BF16)

        links.sent(*core[0])
        for copies in puts + [[put_gbt, put_work]]:
            for copy in copies:
                copy.wait()


def run_fused_feed_forward(lengths, cot, a2, a2t, h1, g1, g2, rows):
    n = cot.shape[1]
    groups, _, _, depth, hidden = g1.shape
    both = (2, Z_DEV, Y_DEV, depth, hidden)
    fold = (2, Z_DEV, depth, hidden)
    return pl.pallas_call(
        fused_feed_forward,
        grid=(groups,),
        in_specs=[SMEM_WHOLE, ANY_WHOLE, VMEM_WHOLE] + [ANY_WHOLE] * 4 + [VMEM_WHOLE],
        out_specs=[ANY_WHOLE, VMEM_WHOLE] + [ANY_WHOLE] * 4 + [VMEM_WHOLE],
        out_shape=[
            shaped(BF16, n, D), shaped(BF16, *fold), shaped(BF16, *both), shaped(F32, n, D),
            shaped(BF16, n, D), shaped(BF16, D, n), shaped(F32, 16, D),
        ],
        scratch_shapes=[
            pltpu.VMEM((n, D), BF16), pltpu.VMEM((D, n), BF16), pltpu.VMEM((n, D), F32),
            pltpu.VMEM((n, D), F32), pltpu.VMEM((n, hidden), BF16), pltpu.VMEM((n, hidden), BF16),
            pltpu.VMEM((2,) + both, BF16),
            pltpu.VMEM((2,) + fold, BF16), pltpu.VMEM(fold, BF16), pltpu.VMEM(both, BF16),
            pltpu.VMEM((2,) + both, BF16),
            pltpu.VMEM(both, BF16), pltpu.VMEM(fold, BF16),
            pltpu.VMEM((D, n), BF16), pltpu.VMEM((n, D), F32), pltpu.VMEM((n, D), BF16),
            pltpu.VMEM(both, BF16),
            pltpu.SemaphoreType.DMA((12,)), pltpu.SemaphoreType.DMA((12,)),
            pltpu.SemaphoreType.DMA((9,)), pltpu.SemaphoreType.DMA((3, n // 256)),
        ],
        compiler_params=pltpu.CompilerParams(
            vmem_limit_bytes=VMEM_LIMIT, collective_id=1, has_side_effects=True
        ),
        name="fused_feed_forward",
    )(lengths, cot, a2, a2t, h1, g1, g2, rows)
class Reduce:
    def __init__(
        self, links, place, work, acc, cross_ref, far_ref, mid_ref, last_ref, side_ref,
        slots=(0, 1), split=False,
    ):
        self.place, self.work, self.acc = place, work, acc
        self.cross_ref, self.far_ref, self.mid_ref = cross_ref, far_ref, mid_ref
        self.last_ref, self.side_ref = last_ref, side_ref
        self.two = len(slots) == 2
        zs = place.zs
        self.y = {
            s: [
                links.add(
                    place.to_y, work(s, zs[j], place.other_y),
                    cross_ref.at[s if self.two else 0, zs[j]],
                )
                for j in (1, 3, 2, 0)
            ]
            for s in slots
        }
        self.z = [
            [
                links.add(place.to_z[1], acc(s, zs[1]), far_ref.at[s, 0]),
                links.add(place.to_z[1], acc(s, zs[3]), far_ref.at[s, 1]),
                links.add(place.to_z[2], mid_ref.at[s, 1], far_ref.at[s, 2]),
            ]
            for s in range(1 if split else 2)
        ]
        self.x = links.add(place.to_x, last_ref, side_ref)

    def fold_y(self, s, half):
        for i, j in [(0, 1), (1, 3), (2, 2), (3, 0)][2 * half : 2 * half + 2]:
            z = self.place.zs[j]
            recv(self.y[s][i])
            value = self.work(s, z, self.place.y)[...].astype(F32)
            cross = self.cross_ref[s if self.two else 0, z].astype(F32)
            self.acc(s, z)[...] = (value + cross).astype(BF16)
            if i < 2:
                start(self.z[s][i])

    def fold_z(self, s):
        recv(self.z[s][:2])
        for i in (1, 0):
            value = self.acc(s, self.place.zs[2 * i])[...].astype(F32)
            self.mid_ref[s, i] = (value + self.far_ref[s, i].astype(F32)).astype(BF16)
            if i:
                start(self.z[s][2])

    def own(self, s):
        recv(self.z[s][2])
        return self.mid_ref[s, 0].astype(F32) + self.far_ref[s, 2].astype(F32)

    def send_x(self):
        self.last_ref[...] = self.own(1).astype(BF16)
        start(self.x)

    def total(self):
        value = self.own(0)
        recv(self.x)
        return value + self.side_ref[...].astype(F32)


class ReduceHalves:
    def __init__(self, links, place, work, landings, last_ref):
        self.place, self.work = place, work
        self.cross, self.far, self.mid, self.far2, self.mid2, self.fin2, self.cross2 = landings
        self.last_ref = last_ref
        zs, half = place.zs, last_ref.shape[0] // 2
        self.low, self.high = pl.ds(0, half), pl.ds(half, half)
        every = slice(None)
        y, other = place.y, place.other_y
        self.y = [
            links.add(place.to_y, work.at[zs[j], other, self.low], self.cross.at[zs[j]])
            for j in (1, 3, 2, 0)
        ]
        self.z = [
            links.add(place.to_z[1], work.at[zs[1], y, self.low], self.far.at[0]),
            links.add(place.to_z[1], work.at[zs[3], y, self.low], self.far.at[1]),
            links.add(place.to_z[2], self.mid.at[1], self.far.at[2]),
        ]
        self.z2 = [
            links.add(place.to_z[1], work.at[zs[1], every, self.high], self.far2.at[0]),
            links.add(place.to_z[1], work.at[zs[3], every, self.high], self.far2.at[1]),
            links.add(place.to_z[2], self.mid2.at[1], self.far2.at[2]),
        ]
        self.y2 = links.add(place.to_y, self.fin2.at[other], self.cross2)

    def begin(self):
        start(self.y, self.z2[:2])

    def add(self, target, left, right):
        target[...] = (left[...].astype(F32) + right[...].astype(F32)).astype(BF16)

    def fold_y(self):
        y, zs = self.place.y, self.place.zs
        for i, j in enumerate((1, 3, 2, 0)):
            recv(self.y[i])
            block = self.work.at[zs[j], y, self.low]
            self.add(block, block, self.cross.at[zs[j]])
            if i < 2:
                start(self.z[i])

    def fold_high(self):
        recv(self.z2[:2])
        for i in (1, 0):
            block = self.work.at[self.place.zs[2 * i], :, self.high]
            self.add(self.mid2.at[i], block, self.far2.at[i])
            if i:
                start(self.z2[2])

    def cross_high(self):
        recv(self.z2[2])
        self.add(self.fin2, self.mid2.at[0], self.far2.at[2])
        start(self.y2)

    def fold_z(self):
        recv(self.z[:2])
        for i in (1, 0):
            block = self.work.at[self.place.zs[2 * i], self.place.y, self.low]
            self.add(self.mid.at[i], block, self.far.at[i])
            if i:
                start(self.z[2])

    def finish(self):
        recv(self.z[2])
        self.add(self.last_ref.at[self.low], self.mid.at[0], self.far.at[2])
        recv(self.y2)
        self.add(self.last_ref.at[self.high], self.fin2.at[self.place.y], self.cross2)


def fused_backward(
    tokens_ref, gq_in, gw_in, rows_ref, dh1_ref, gb_ref, gbt_in, q_in, v_in, kt_in,
    p_ref, scale_in, o_in, a1t_in, layer_in, fold_in, work_in, early_ref,
    out_ref, layerout_ref, part0_ref, partw_ref, part1_ref, part2_ref, total_ref,
    gq_ref, gw_ref, q_ref, v_ref, kt_ref, scale_ref, o_ref,
    a1t_ref, gbt_ref, layer_ref, fold_ref, work_ref, do_ref, delta_ref, dkv_ref, dqkv_ref, da1_ref, own_ref, passing_ref, passlayer_ref, bqv_ref,
    folded_ref, cross1_ref, far1_ref, mid1_ref, last1_ref, side1_ref,
    cross2_ref, far2_ref, mid2_ref, last2_ref, side2_ref,
    stagew_ref, landw_ref, workw_ref, crossw_ref, farw_ref, midw_ref, lastw_ref, sidew_ref,
    stage0_ref, land0_ref, work0_ref, cross0_ref, far0_ref, mid0_ref, last0_ref, side0_ref,
    sums_ref, sumland_ref,
    send_sem, recv_sem, local_sem, result_sem, group_sem, *tail_refs,
):
    t = pl.program_id(0)
    n = own_ref.shape[0]
    width = gw_ref.shape[-1]
    depth = part0_ref.shape[0]
    heads = width // HEAD_DIM
    step = n // 4
    place = Place()
    y = place.y
    links = Links(send_sem, recv_sem)
    k, i = group_and_block(t)
    mine = place.group(k)
    now = k % 2
    out = Result(links, place, own_ref, passing_ref, out_ref, step, result_sem.at[0], 4)
    layer = Result(links, place, layer_ref, passlayer_ref, layerout_ref, step, result_sem.at[1], 4)
    fetch = pltpu.make_async_copy(tokens_ref.at[place.t], own_ref, local_sem.at[0])
    fetch_layer, fetch_work, fetch_fold, fetch_gbt, fetch_a1t = [
        pltpu.make_async_copy(there, here, local_sem.at[1 + j])
        for j, (there, here) in enumerate([
            (layer_in, layer_ref), (work_in, work_ref), (fold_in, fold_ref),
            (gbt_in, gbt_ref), (a1t_in, a1t_ref),
        ])
    ]
    def operands(group):
        slot = group % 2
        pairs = [
            (gw_in, gw_ref), (scale_in, scale_ref), (o_in, o_ref), (v_in, v_ref),
            (q_in, q_ref), (kt_in, kt_ref), (gq_in, gq_ref),
        ]
        return [
            pltpu.make_async_copy(there.at[group], here.at[slot], group_sem.at[slot, j])
            for j, (there, here) in enumerate(pairs)
        ]

    corew = [links.add(place.to_core, stagew_ref, landw_ref.at[i]) for i in range(2)]
    core0 = [links.add(place.to_core, stage0_ref, land0_ref.at[i]) for i in range(2)]
    def half_done(i, *landing):
        return Reduce(
            links, place, lambda s, z, y: work_ref.at[i, z, y],
            lambda s, z: folded_ref.at[i, z] if s else fold_ref.at[i, z],
            *landing, slots=(1,),
        )

    seg1 = half_done(0, cross1_ref, far1_ref, mid1_ref, last1_ref, side1_ref)
    seg2 = half_done(1, cross2_ref, far2_ref, mid2_ref, last2_ref, side2_ref)
    segw = Reduce(
        links, place, lambda s, z, y: workw_ref.at[s, z, y],
        lambda s, z: workw_ref.at[s, z, y],
        crossw_ref, farw_ref, midw_ref, lastw_ref, sidew_ref,
    )
    seg0 = Reduce(
        links, place, lambda s, z, y: work0_ref.at[s, z, y],
        lambda s, z: work0_ref.at[s, z, y],
        cross0_ref, far0_ref, mid0_ref, last0_ref, side0_ref, slots=(0,), split=True,
    )
    tail = ReduceHalves(links, place, work0_ref.at[1], tail_refs, last0_ref)
    sum_core, sum_y, *sum_z, sum_x = [
        links.add(to, sums_ref.at[i], sumland_ref.at[j])
        for j, (i, to) in enumerate(
            zip([0, 1, 2, 2, 2, 3], [place.to_core, place.to_y] + place.to_z[1:] + [place.to_x])
        )
    ]

    early_copies = [
        corew[1], core0[1], *segw.y[0], *segw.y[1], *segw.z[0], *seg0.y[0], *seg0.z[0],
        out.x[3], out.core[3], *layer.x, *layer.core, *layer.far, seg1.x, seg2.x,
    ]
    for seg in (seg1, seg2):
        early_copies += [*seg.y[1], *seg.z[0], *seg.z[1]]

    def sent(copies):
        for copy in copies:
            copy.wait_send()

    def when(point):
        return pl.when(t == point)

    @when(0)
    def _():
        start(fetch_layer, operands(1), fetch_work, fetch_fold, fetch_gbt, operands(0))
        start(fetch, fetch_a1t)
        place.greet()
        fetch_layer.wait()
        for i in range(4):
            layer.send(i)
        fetch_work.wait()
        start(seg1.y[1], seg2.y[1])
        fetch_fold.wait()
        start(seg1.z[0][:2], seg2.z[0][:2])
        bqv_ref[...] = jnp.zeros_like(bqv_ref)
        sums_ref[0] = early_ref[...]
        fetch_gbt.wait()

    def add_core():
        recv(corew[1])

        @pl.loop(0, Z_DEV)
        def _(z):
            workw_ref[1, z] = (
                workw_ref[1, z].astype(F32) + landw_ref[1, z].astype(F32)
            ).astype(BF16)

        start(segw.y[1])

    def wait(copies):
        for copy in copies:
            copy.wait()

    @when(0)
    def _():
        wait(operands(1))

    @when(4)
    def _():
        start(operands(3))
        wait(operands(0))

    @when(8)
    def _():
        start(operands(2))
        wait(operands(3))

    @when(9)
    def _():
        wait(operands(2))

    plan = [
        (2, 1, lambda: (seg1.fold_y(1, 0), seg1.fold_z(0))),
        (3, 1, lambda: layer.pass_on(0)),
        (4, 0, lambda: (seg1.fold_y(1, 1), seg2.fold_z(0))),
        (4, 1, lambda: layer.pass_on(1)),
        (5, 1, lambda: (seg1.fold_z(1), seg2.fold_y(1, 0))),
        (8, 0, lambda: (seg2.fold_y(1, 1), layer.pass_on(2))),
        (8, 1, lambda: (seg1.send_x(), segw.fold_y(0, 0), segw.fold_y(0, 1))),
        (9, 0, add_core),
        (9, 1, lambda: (seg2.fold_z(1), seg0.fold_y(0, 0), layer.pass_on(3))),
        (10, 1, lambda: segw.fold_z(0)),
        (11, 1, lambda: (seg2.send_x(), seg0.fold_y(0, 1))),
        (12, 1, lambda: (segw.fold_y(1, 0), segw.fold_y(1, 1))),
        (13, 1, lambda: (seg0.fold_z(0), out.pass_on(3))),
        (14, 1, lambda: segw.fold_z(1)),
    ]

    def serve(point):
        for at, where, act in plan:
            if where == point:
                pl.when(t == at)(lambda act=act: (act(), None)[1])

    @pl.when((t == 0) | (t == 4) | (t == 8) | (t == 9))
    def _():
        pick = (
            lax.broadcasted_iota(jnp.int32, (8, width), 1) // HEAD_DIM
            == lax.broadcasted_iota(jnp.int32, (8, width), 0)
        ).astype(BF16)

        @pl.loop(0, n // step)
        def _(i):
            rows = pl.ds(pl.multiple_of(i * step, step), step)
            columns = scale_ref[now, :, rows].T
            lane = lax.broadcasted_iota(jnp.int32, (step, width), 1)
            scale = columns[:, heads - 1 : heads]
            for h in reversed(range(heads - 1)):
                scale = jnp.where(lane < (h + 1) * HEAD_DIM, columns[:, h : h + 1], scale)
            do = (dot_nn(gb_ref[rows, :], gw_ref[now]) * scale).astype(BF16)
            do_ref[now, rows, :] = do
            product = do.astype(F32) * o_ref[now, rows, :].astype(F32)
            high = product.astype(BF16)
            low = (product - high.astype(F32)).astype(BF16)
            delta_ref[now, :, rows] = dot_nt(pick, high) + dot_nt(pick, low)

        value = dot_nn(gbt_ref[...], o_ref[now]).reshape(Z_DEV, Y_DEV, depth, width)
        for s in range(2):
            @when(8 * s)
            def _():
                if s:
                    corew[0].wait_send()
                stagew_ref[...] = value.astype(BF16)
                start(corew[s])

        @when(4)
        def _():
            recv(corew[0])
            workw_ref[0] = (value + landw_ref[0].astype(F32)).astype(BF16)
            start(segw.y[0])

        @when(9)
        def _():
            workw_ref[1] = value.astype(BF16)

    serve(0)

    for ii in reversed(range(4)):
        @pl.when(i == ii)
        def _():
            first, last = ii * step, (ii + 1) * step
            do = do_ref[now, first:last, :]
            q = q_ref[now, first:last, :]
            v = v_ref[now, :last, :]
            lane = lax.broadcasted_iota(jnp.int32, (1, width), 1)
            dk, dv, dq = None, None, []
            for h in range(heads):
                low, high = h * HEAD_DIM, (h + 1) * HEAD_DIM
                here = (lane >= low) & (lane < high)
                p = p_ref[0, h, 0, :last, :]
                dp = dot_nt(v, jnp.where(here, do, jnp.zeros((), BF16)))
                ds = p * (dp - delta_ref[now, h : h + 1, first:last]).astype(BF16)
                part = dot_nn(p, do)
                dv = part if dv is None else jnp.where(lane < low, dv, part)
                part = dot_nn(ds, q)
                dk = part if dk is None else jnp.where(lane < low, dk, part)
                dq.append(dot_nn(kt_ref[now, low:high, :last], ds))
            if ii == 3:
                dkv_ref[now, 0] = dk
                dkv_ref[now, 1] = dv
            else:
                dkv_ref[now, 0, :last, :] += dk
                dkv_ref[now, 1, :last, :] += dv
            dk = dkv_ref[now, 0, first:last, :].astype(BF16)
            dv = dkv_ref[now, 1, first:last, :].astype(BF16)
            dq = (jnp.concatenate(dq, 0) * HEAD_DIM ** -0.5).astype(BF16).T
            dqkv_ref[now, first:last, :width] = dq
            dqkv_ref[now, first:last, width : 2 * width] = dk
            dqkv_ref[now, first:last, 2 * width :] = dv
            bqv_ref[mine, 0:1, :] += jnp.sum(dq.astype(F32), 0, keepdims=True)
            bqv_ref[mine, 1:2, :] += jnp.sum(dv.astype(F32), 0, keepdims=True)

            @pl.when(t >= 8)
            def _():
                da1_ref[first:last, :] += dot_nt(dqkv_ref[now, first:last, :], gq_ref[now])

    serve(1)

    @pl.when((t == 3) | (t == 7) | (t > 13))
    def _():
        @when(3)
        def _():
            fetch.wait()
            fetch_a1t.wait()

        @when(3)
        def _():
            da1_ref[...] = dot_nt(dqkv_ref[now], gq_ref[now])

        @when(7)
        def _():
            da1_ref[...] += dot_nt(dqkv_ref[now], gq_ref[now])

        value = dot_nn(a1t_ref[...], dqkv_ref[now]).reshape(Z_DEV, Y_DEV, depth, 3 * width)
        for s in range(2):
            @when(3 + 11 * s)
            def _():
                if s:
                    core0[0].wait_send()
                stage0_ref[...] = value.astype(BF16)
                start(core0[s])

            @when(7 + 8 * s)
            def _():
                recv(core0[s])
                work0_ref[s] = (value + land0_ref[s].astype(F32)).astype(BF16)
                if s:
                    tail.begin()
                else:
                    start(seg0.y[s])

    @pl.when((t > 8) & (t % 2 == 1))
    def _():
        rows = pl.ds(pl.multiple_of(i * step, step), step)
        xhat, r = norm_parts(own_ref[rows, :].astype(F32))
        da1 = da1_ref[rows, :]
        sums_ref[0, 0:1, :] += jnp.sum(da1 * xhat, 0, keepdims=True)
        sums_ref[0, 2:3, :] += jnp.sum(da1, 0, keepdims=True)
        dg = da1 * rows_ref[0:1, :]
        dv = r * (
            dg
            - jnp.mean(dg, -1, keepdims=True)
            - xhat * jnp.mean(dg * xhat, -1, keepdims=True)
        )
        own_ref[rows, :] = (dh1_ref[...] + dv).astype(BF16)
        for ii in range(4):
            @pl.when(i == ii)
            def _():
                out.send(ii)

    @when(15)
    def _():
        for s in range(4):
            sums_ref[0, 3:5, s * width : (s + 1) * width] = bqv_ref[s, 0:2, :]
        start(sum_core)
        segw.send_x()
        tail.fold_high()
        recv(sum_core)
        sums_ref[1] = sums_ref[0] + sumland_ref[0]
        start(sum_y)
        tail.fold_y()
        tail.cross_high()
        out.pass_on(2)
        tail.fold_z()
        out.pass_on(1)
        recv(sum_y)
        sums_ref[2] = sums_ref[1] + sumland_ref[1]
        start(sum_z)
        tail.finish()
        start(seg0.x)
        part1_ref[...] = seg1.total()
        part2_ref[...] = seg2.total()
        recv(sum_z)
        sums_ref[3] = (sums_ref[2] + sumland_ref[2]) + (sumland_ref[3] + sumland_ref[4])
        start(sum_x)
        sent(early_copies)
        out.pass_on(0)
        partw_ref[...] = segw.total()
        layer.finish()
        recv(sum_x)
        total_ref[...] = sums_ref[3] + sumland_ref[5]
        part0_ref[...] = seg0.total()
        out.finish()
        links.sent(corew[0], core0[0], *early_copies)


def group_and_block(t):
    early = t < 8
    return (
        jnp.where(early, 1 - t // 4, 3 - t % 2),
        3 - jnp.where(early, t % 4, jnp.maximum(t - 8, 0) // 2),
    )


def run_fused_backward(
    tokens, gq, gw, rows, dh1, gb, gbt, q, v, kt, p, scale, o, a1t, layer, fold, work, early
):
    groups, n, _ = tokens.shape
    width = gw.shape[-1]
    heads = width // HEAD_DIM
    hidden = fold.shape[-1]
    depth = D // (Z_DEV * Y_DEV)
    step = n // 4

    p_spec = pl.BlockSpec(
        (1, heads, 1, n, step),
        lambda t: (group_and_block(t)[0], 0, group_and_block(t)[1], 0, 0),
    )

    copies = 12 + 12 + 4 + 15 + 2 * 11 + 8 + 11 + 6

    def landing(lanes, slots=1):
        return [
            pltpu.VMEM((slots, Z_DEV, depth, lanes), BF16),
            pltpu.VMEM((2, 3, depth, lanes), BF16), pltpu.VMEM((2, 2, depth, lanes), BF16),
            pltpu.VMEM((depth, lanes), BF16), pltpu.VMEM((depth, lanes), BF16),
        ]

    def working(lanes):
        block = (Z_DEV, Y_DEV, depth, lanes)
        return [pltpu.VMEM(block, BF16)] + [pltpu.VMEM((2,) + block, BF16)] * 2

    return pl.pallas_call(
        fused_backward,
        grid=(4 * groups,),
        in_specs=[
            ANY_WHOLE, ANY_WHOLE, ANY_WHOLE, VMEM_WHOLE,
            pl.BlockSpec((step, D), lambda t: (group_and_block(jnp.maximum(t, 8))[1], 0)),
            VMEM_WHOLE, ANY_WHOLE, ANY_WHOLE, ANY_WHOLE, ANY_WHOLE, p_spec,
            ANY_WHOLE, ANY_WHOLE, ANY_WHOLE, ANY_WHOLE, ANY_WHOLE, ANY_WHOLE, VMEM_WHOLE,
        ],
        out_specs=[ANY_WHOLE] * 2 + [VMEM_WHOLE] * 5,
        out_shape=[
            shaped(BF16, groups, n, D), shaped(BF16, groups, n, D),
            shaped(F32, depth, 3 * width),
            shaped(F32, depth, width), shaped(F32, depth, hidden),
            shaped(F32, depth, hidden), shaped(F32, 16, D),
        ],
        scratch_shapes=[
            pltpu.VMEM((2, D, 3 * width), BF16), pltpu.VMEM((2, D, width), BF16),
            pltpu.VMEM((2, n, width), BF16), pltpu.VMEM((2, n, width), BF16),
            pltpu.VMEM((2, width, n), BF16), pltpu.VMEM((2, 8, n), F32),
            pltpu.VMEM((2, n, width), BF16),
            pltpu.VMEM((D, n), BF16), pltpu.VMEM((D, n), BF16), pltpu.VMEM((n, D), BF16),
            pltpu.VMEM((2, Z_DEV, depth, hidden), BF16),
            pltpu.VMEM((2, Z_DEV, Y_DEV, depth, hidden), BF16),
            pltpu.VMEM((2, n, width), BF16),
            pltpu.VMEM((2, 8, n), F32), pltpu.VMEM((2, 2, n, width), F32),
            pltpu.VMEM((2, n, 3 * width), BF16), pltpu.VMEM((n, D), F32),
            pltpu.VMEM((n, D), BF16), pltpu.VMEM((n, D), BF16), pltpu.VMEM((n, D), BF16),
            pltpu.VMEM((groups, 8, width), F32),
        ]
        + [pltpu.VMEM((2, Z_DEV, depth, hidden), BF16)] + landing(hidden) + landing(hidden)
        + working(width) + landing(width, 2)
        + working(3 * width) + landing(3 * width)
        + [
            pltpu.VMEM((4, 16, D), F32), pltpu.VMEM((6, 16, D), F32),
            pltpu.SemaphoreType.DMA((copies,)), pltpu.SemaphoreType.DMA((copies,)),
            pltpu.SemaphoreType.DMA((6,)), pltpu.SemaphoreType.DMA((2, 2, 4)),
            pltpu.SemaphoreType.DMA((2, 7)),
            pltpu.VMEM((Z_DEV, depth // 2, 3 * width), BF16),
            pltpu.VMEM((3, depth // 2, 3 * width), BF16),
            pltpu.VMEM((2, depth // 2, 3 * width), BF16),
            pltpu.VMEM((3, Y_DEV, depth // 2, 3 * width), BF16),
            pltpu.VMEM((2, Y_DEV, depth // 2, 3 * width), BF16),
            pltpu.VMEM((Y_DEV, depth // 2, 3 * width), BF16),
            pltpu.VMEM((depth // 2, 3 * width), BF16),
        ],
        compiler_params=pltpu.CompilerParams(
            vmem_limit_bytes=VMEM_LIMIT, collective_id=2, has_side_effects=True
        ),
        name="fused_backward",
    )(tokens, gq, gw, rows, dh1, gb, gbt, q, v, kt, p, scale, o, a1t, layer, fold, work, early)


def place_gradients(
    tie_ref, sums_ref, part0_ref, partw_ref, part1_ref, part2_ref, near_out_ref,
    near_grad_ref, far_out_ref, far_grad_ref, gains_ref, bias_ref, in_ref, out_ref, expand_ref,
    project_ref, chosen_ref,
):
    t = pl.program_id(0)
    far_out_ref[...] = near_out_ref[...]
    far_grad_ref[...] = near_grad_ref[...]
    own = gains_ref.shape[-1]
    width = partw_ref.shape[-1]
    kinds = [tie_ref[0], tie_ref[1], tie_ref[2], tie_ref[3]]

    @pl.when(t == 0)
    def _():
        first = (lax.axis_index("dp") * 4 + lax.axis_index("tensor")) * own
        feature = lax.broadcasted_iota(jnp.int32, (D, 128), 0)
        lane = lax.broadcasted_iota(jnp.int32, (D, 128), 1)
        chosen = ((feature == first + lane) & (lane < own)).astype(F32)
        chosen_ref[...] = lax.dot_general(
            sums_ref[...], chosen, (((1,), (0,)), ((), ())),
            precision=lax.Precision.HIGHEST, preferred_element_type=F32,
        )
        row = lax.broadcasted_iota(jnp.int32, (NSRC, own), 0)
        for i, kind in enumerate([0, 0, 0, 1, 2, 3, 2, 2, 2, 2]):
            value = chosen_ref[2 + i : 3 + i, :own]
            bias_ref[i] = jnp.where(row == kinds[kind], value, 0.0)

    @pl.when(t < NSRC)
    def _():
        def here(kind, value):
            return jnp.where(kinds[kind] == t, value, jnp.zeros_like(value))

        gains_ref[0, 0:1] = here(0, chosen_ref[0:1, :own])
        gains_ref[0, 1:2] = here(2, chosen_ref[1:2, :own])
        for j in range(3):
            in_ref[0, j] = here(0, part0_ref[:, j * width : (j + 1) * width])
        out_ref[0] = here(1, partw_ref[...].T)
        expand_ref[0] = here(2, part1_ref[...])
        project_ref[0] = here(3, part2_ref[...])


def run_place_gradients(tie, sums, part0, partw, part1, part2, out, grad, like):
    slots, n, _ = grad.shape
    gains, biases, w_in, w_out, w_expand, w_project = [item.shape for item in like]
    shapes = [
        gains, (biases[1], biases[0], biases[2]), w_in, w_out, w_expand,
        (w_project[0], w_project[2], w_project[1]),
    ]

    def source(shape):
        return pl.BlockSpec(
            (1,) + shape[1:], lambda t: (jnp.minimum(t, NSRC - 1),) + (0,) * (len(shape) - 1)
        )

    out, grad, gains, biases, w_in, w_out, w_expand, w_project = pl.pallas_call(
        place_gradients,
        grid=(slots,),
        in_specs=[SMEM_WHOLE] + [VMEM_WHOLE] * 5 + [group(n, D), group(n, D)],
        out_specs=[group(n, D), group(n, D), source(shapes[0]), VMEM_WHOLE]
        + [source(shape) for shape in shapes[2:]],
        out_shape=[shaped(BF16, slots, n, D)] * 2 + [shaped(F32, *item) for item in shapes],
        scratch_shapes=[pltpu.VMEM((16, 128), F32)],
        compiler_params=pltpu.CompilerParams(vmem_limit_bytes=VMEM_LIMIT),
        name="place_gradients",
    )(tie, sums, part0, partw, part1, part2, out, grad)
    biases = biases.transpose(1, 0, 2)
    return out, grad, gains, biases, w_in, w_out, w_expand, w_project.transpose(0, 2, 1)


def plain_step(
    tokens, lengths, tie_map, norm_gains, bias_rows, attention_in, attention_out,
    expand_weight, project_weight, cotangent,
):
    slot_rows = tokens.shape[0] // lengths.shape[0]
    me = lax.axis_index("tensor")
    in_local = lax.dynamic_index_in_dim(attention_in, tie_map[0], 0, keepdims=False)
    out_local = lax.dynamic_index_in_dim(attention_out, tie_map[1], 0, keepdims=False)
    expand_local = lax.dynamic_index_in_dim(expand_weight, tie_map[2], 0, keepdims=False)
    project_local = lax.dynamic_index_in_dim(project_weight, tie_map[3], 0, keepdims=False)
    local0 = jnp.concatenate([in_local, out_local.T[None]], 0)
    row_kinds = jnp.array([0, 0, 0, 1, 2, 3] + [2] * (FF // D), dtype=jnp.int32)
    gain_kinds = jnp.array([0, 2], dtype=jnp.int32)
    gain_pick = norm_gains[tie_map[gain_kinds], jnp.arange(2)]
    bias_pick = bias_rows[tie_map[row_kinds], jnp.arange(row_kinds.shape[0])]
    vectors = jnp.concatenate([gain_pick, bias_pick], 0)
    x = lax.dynamic_slice_in_dim(tokens, me * slot_rows, slot_rows, 0)
    cot = lax.dynamic_slice_in_dim(cotangent, me * slot_rows, slot_rows, 0)
    length = lax.dynamic_slice_in_dim(lengths, me, 1, 0)
    rows = lax.all_gather(vectors, ("dp", "tensor"), axis=1, tiled=True).astype(F32)
    rows = jnp.concatenate([rows, jnp.zeros((4, D), F32)], 0)

    def gathered(piece, axis):
        piece = lax.all_gather(piece, "dp", axis=axis, tiled=True)
        return lax.all_gather(piece, "tensor", axis=0)

    g0 = gathered(local0, 1)
    g1 = gathered(expand_local, 0)
    g2 = gathered(project_local.T, 0)
    groups, width = g0.shape[0], g0.shape[-1]
    bqv = rows[3:5].reshape(2, groups, width).transpose(1, 0, 2)
    q, v, kt, p, o, a1t, h1, a2, a2t = run_attention_forward(length, x, g0, rows, bqv)
    out, d1, d2, dh1, gb, gbt, sums = run_feed_forward(length, cot, a2, a2t, h1, g1, g2, rows)
    d0, xg, sums_in, sums_qv = run_attention_backward(
        x, g0, rows, dh1, gb, gbt, q, v, kt, p, o, a1t
    )
    layer_out = lax.all_gather(out, "tensor", axis=0, tiled=True)
    tokens_grad = lax.all_gather(xg, "tensor", axis=0, tiled=True)

    def scattered(piece, axis):
        piece = lax.psum_scatter(piece, "tensor", scatter_dimension=0)
        return lax.psum_scatter(piece, "dp", scatter_dimension=axis, tiled=True).astype(F32)

    part0 = scattered(d0, 1)
    part1 = scattered(d1, 0)
    part2 = scattered(d2, 0)
    qv = sums_qv[:, :2].transpose(1, 0, 2).reshape(2, D)
    sums = jnp.concatenate(
        [sums_in[0:1], sums[1:2], sums_in[1:2], qv, sums[5:12]], 0
    )
    sums = lax.psum_scatter(sums, ("dp", "tensor"), scatter_dimension=1, tiled=True)
    return layer_out, tokens_grad, *placed(tie_map, sums, part0, part1, part2)


def fused_step(
    tokens, lengths, tie_map, norm_gains, bias_rows, attention_in, attention_out,
    expand_weight, project_weight, cotangent,
):
    slots = lengths.shape[0]
    tokens = tokens.reshape(slots, -1, D)
    cotangent = cotangent.reshape(slots, -1, D)
    gq, gw, g1, g2, rows, q, v, kt, p, scale, o, a1t, h1, a2, a2t = run_fused_forward(
        tie_map, lengths, tokens, norm_gains, bias_rows, attention_in, attention_out,
        expand_weight, project_weight,
    )
    layer, fold, work, dh1, gb, gbt, early = run_fused_feed_forward(
        lengths, cotangent, a2, a2t, h1, g1, g2, rows
    )
    grad, out, part0, partw, part1, part2, sums = run_fused_backward(
        tokens, gq, gw, rows, dh1, gb, gbt, q, v, kt, p, scale, o, a1t, layer, fold,
        work, early,
    )
    out, grad, *placed_grads = run_place_gradients(
        tie_map, sums, part0, partw, part1, part2, out, grad,
        (norm_gains, bias_rows, attention_in, attention_out, expand_weight, project_weight),
    )
    return out.reshape(-1, D), grad.reshape(-1, D), *placed_grads


def placed(tie_map, sums, part0, part1, part2):
    source = jnp.arange(NSRC, dtype=jnp.int32)

    def place(piece, which):
        pick = (source == tie_map[which]).reshape((NSRC,) + (1,) * piece.ndim)
        return jnp.where(pick, piece[None], 0.0)

    def place_rows(piece, kinds):
        pick = source[:, None] == tie_map[jnp.array(kinds, dtype=jnp.int32)][None, :]
        return jnp.where(pick[:, :, None], piece[None], 0.0)

    return (
        place_rows(sums[:2], [0, 2]),
        place_rows(sums[2:], [0, 0, 0, 1, 2, 3] + [2] * (FF // D)),
        place(part0[:3], 0),
        place(part0[3].T, 1),
        place(part1, 2),
        place(part2.T, 3),
    )


def solution(mesh):
    fused = mesh.shape["dp"] == Z_DEV * Y_DEV and mesh.shape["tensor"] == X_DEV * C_DEV
    return jax.shard_map(
        fused_step if fused else plain_step,
        mesh=mesh,
        in_specs=(
            P("dp", None),
            P("dp"),
            P(),
            P(None, None, ("dp", "tensor")),
            P(None, None, ("dp", "tensor")),
            P(None, None, "dp", "tensor"),
            P(None, "tensor", "dp"),
            P(None, "dp", "tensor"),
            P(None, "tensor", "dp"),
            P("dp", None),
        ),
        out_specs=(
            P("dp", None),
            P("dp", None),
            P(None, None, ("dp", "tensor")),
            P(None, None, ("dp", "tensor")),
            P(None, None, "dp", "tensor"),
            P(None, "tensor", "dp"),
            P(None, "dp", "tensor"),
            P(None, "tensor", "dp"),
        ),
        check_vma=False,
    )
```

```python
import jax
import jax.numpy as jnp
from jax import lax
from jax.experimental import pallas as pl
from jax.experimental.pallas import tpu as pltpu
from jax.sharding import PartitionSpec as P

D = 768
HEAD_DIM = 64
FF = 3072
NSRC = 4
EPS = 1e-05
MASKED = -1e30
F32 = jnp.float32
BF16 = jnp.bfloat16
VMEM_LIMIT = 60 * 1024 * 1024


def dot_nn(a, b):
    return lax.dot_general(a, b, (((1,), (0,)), ((), ())), preferred_element_type=F32)


def dot_nt(a, b):
    return lax.dot_general(a, b, (((1,), (1,)), ((), ())), preferred_element_type=F32)


def norm_parts(v):
    center = jnp.mean(v, -1, keepdims=True)
    centered = v - center
    r = lax.rsqrt(jnp.mean(centered * centered, -1, keepdims=True) + EPS)
    return centered * r, r


def head_mask(shape, h):
    lane = lax.broadcasted_iota(jnp.int32, shape, 1)
    return (lane >= h * HEAD_DIM) & (lane < (h + 1) * HEAD_DIM)


def blocks(total, size):
    return [slice(i * size, (i + 1) * size) for i in range(total // size)]


def attention_forward(
    len_ref, x_ref, g_ref, rows_ref, bqv_ref,
    q_ref, v_ref, kt_ref, p_ref, o_ref, a1t_ref, h1_ref, a2_ref, a2t_ref,
    a1_ref, k_ref, vt_ref, ot_ref, attn_ref,
):
    t = pl.program_id(0)
    n = x_ref.shape[0]
    width = g_ref.shape[-1]
    heads = width // HEAD_DIM
    step = 256
    length = len_ref[0]

    @pl.when(t == 0)
    def _():
        @pl.loop(0, n // step)
        def _(b):
            rows = pl.ds(pl.multiple_of(b * step, step), step)
            xhat, _ = norm_parts(x_ref[rows, :].astype(F32))
            a1 = xhat * rows_ref[0:1, :] + rows_ref[2:3, :]
            a1_ref[rows, :] = a1.astype(BF16)
            a1t_ref[:, rows] = a1.astype(BF16).T
            attn_ref[rows, :] = x_ref[rows, :].astype(F32) + rows_ref[5:6, :]

    @pl.loop(0, n // step)
    def _(b):
        rows = pl.ds(pl.multiple_of(b * step, step), step)
        a1 = a1_ref[rows, :]
        q = (dot_nn(a1, g_ref[0, 0]) + bqv_ref[0, 0:1, :]).astype(BF16)
        q_ref[0, rows, :] = q * jnp.asarray(HEAD_DIM ** -0.5, BF16)
        k = dot_nn(a1, g_ref[0, 1]).astype(BF16)
        k_ref[rows, :] = k
        kt_ref[0, :, rows] = k.T
        v = (dot_nn(a1, g_ref[0, 2]) + bqv_ref[0, 1:2, :]).astype(BF16)
        v_ref[0, rows, :] = v
        vt_ref[:, rows] = v.T

    for h in range(heads):
        k = k_ref[...]
        k = jnp.where(head_mask(k.shape, h), k, jnp.zeros_like(k))
        for b in range(n // step):
            first, last = b * step, (b + 1) * step
            q = q_ref[0, first:last, :]
            key = lax.broadcasted_iota(jnp.int32, (last, step), 0)
            query = lax.broadcasted_iota(jnp.int32, (step, step), 1) + first
            s = dot_nt(k[:last], q)
            near = jnp.where(
                (key[first:] <= query) & (key[first:] < length), s[first:], MASKED
            )
            if b:
                far = jnp.where(key[:first] < length, s[:first], MASKED)
                top = jnp.maximum(
                    jnp.max(far, 0, keepdims=True), jnp.max(near, 0, keepdims=True)
                )
                e_far = jnp.exp(far - top)
                e_near = jnp.exp(near - top)
                total = jnp.sum(e_far, 0, keepdims=True) + jnp.sum(e_near, 0, keepdims=True)
                scale = 1.0 / total
                p_ref[0, h, :first, first:last] = (e_far * scale).astype(BF16)
            else:
                top = jnp.max(near, 0, keepdims=True)
                e_near = jnp.exp(near - top)
                scale = 1.0 / jnp.sum(e_near, 0, keepdims=True)
            p_ref[0, h, first:last, first:last] = (e_near * scale).astype(BF16)
            ot_ref[h * HEAD_DIM : (h + 1) * HEAD_DIM, first:last] = dot_nn(
                vt_ref[h * HEAD_DIM : (h + 1) * HEAD_DIM, :last],
                p_ref[0, h, :last, first:last],
            ).astype(BF16)

    @pl.loop(0, n // step)
    def _(b):
        rows = pl.ds(pl.multiple_of(b * step, step), step)
        o = ot_ref[:, rows].T
        o_ref[0, rows, :] = o
        attn_ref[rows, :] += dot_nt(o, g_ref[0, 3])

    @pl.when(t == pl.num_programs(0) - 1)
    def _():
        @pl.loop(0, n // step)
        def _(b):
            rows = pl.ds(pl.multiple_of(b * step, step), step)
            h1 = attn_ref[rows, :]
            h1_ref[rows, :] = h1
            xhat, _ = norm_parts(h1)
            a2 = (xhat * rows_ref[1:2, :] + rows_ref[6:7, :]).astype(BF16)
            a2_ref[rows, :] = a2
            a2t_ref[:, rows] = a2.T


SQRT_2_PI = 0.7978845608028654


def feed_forward_both(
    len_ref, c_ref, a2_ref, a2t_ref, h1_ref, w1_ref, w2_ref, rows_ref,
    out_ref, d1_ref, d2_ref, dh1_ref, gb_ref, gbt_ref, sums_ref,
    gf_ref, gft_ref, feed_ref, da2_ref, h_ref, df_ref,
):
    t = pl.program_id(0)
    n = c_ref.shape[0]
    step = 256
    length = len_ref[0]

    @pl.when(t == 0)
    def _():
        sums_ref[...] = jnp.zeros_like(sums_ref)

        @pl.loop(0, n // step)
        def _(b):
            rows = pl.ds(pl.multiple_of(b * step, step), step)
            place = b * step + lax.broadcasted_iota(jnp.int32, (step, 1), 0)
            live = (place < length).astype(F32)
            g = (c_ref[rows, :].astype(F32) * live).astype(BF16)
            gf_ref[rows, :] = g
            gft_ref[:, rows] = g.T
            sums_ref[7:8, :] += jnp.sum(g.astype(F32), 0, keepdims=True)

    bias = rows_ref[pl.ds(8 + t, 1), :]

    @pl.loop(0, n // step)
    def _(b):
        rows = pl.ds(pl.multiple_of(b * step, step), step)
        f = dot_nn(a2_ref[rows, :], w1_ref[0]) + bias
        dh = dot_nn(gf_ref[rows, :], w2_ref[0])
        f2 = f * f
        th = jnp.tanh(f * (SQRT_2_PI + (SQRT_2_PI * 0.044715) * f2))
        half = 0.5 + 0.5 * th
        h = (f * half).astype(BF16)
        slope = half + f * (0.5 - 0.5 * th * th) * (
            SQRT_2_PI + (3 * SQRT_2_PI * 0.044715) * f2
        )
        df = (dh * slope).astype(BF16)
        h_ref[rows, :] = h
        df_ref[rows, :] = df
        sums_ref[pl.ds(8 + t, 1), :] += jnp.sum(df.astype(F32), 0, keepdims=True)
        feed = dot_nt(h, w2_ref[0])
        da2 = dot_nt(df, w1_ref[0])

        @pl.when(t == 0)
        def _():
            feed_ref[rows, :] = feed
            da2_ref[rows, :] = da2

        @pl.when(t > 0)
        def _():
            feed_ref[rows, :] += feed
            da2_ref[rows, :] += da2

    @pl.loop(0, D // step)
    def _(b):
        rows = pl.ds(pl.multiple_of(b * step, step), step)
        d1_ref[0, rows, :] = dot_nn(a2t_ref[rows, :], df_ref[...]).astype(BF16)
        d2_ref[0, rows, :] = dot_nn(gft_ref[rows, :], h_ref[...]).astype(BF16)

    @pl.when(t == pl.num_programs(0) - 1)
    def _():
        @pl.loop(0, n // step)
        def _(b):
            rows = pl.ds(pl.multiple_of(b * step, step), step)
            place = b * step + lax.broadcasted_iota(jnp.int32, (step, 1), 0)
            live = (place < length).astype(F32)
            h1 = h1_ref[rows, :]
            out_ref[rows, :] = (live * (h1 + (feed_ref[rows, :] + rows_ref[7:8, :]))).astype(BF16)
            xhat, r = norm_parts(h1)
            da2 = da2_ref[rows, :]
            sums_ref[1:2, :] += jnp.sum(da2 * xhat, 0, keepdims=True)
            sums_ref[6:7, :] += jnp.sum(da2, 0, keepdims=True)
            dg = da2 * rows_ref[1:2, :]
            dv = r * (
                dg
                - jnp.mean(dg, -1, keepdims=True)
                - xhat * jnp.mean(dg * xhat, -1, keepdims=True)
            )
            dh1 = live * c_ref[rows, :].astype(F32) + dv
            dh1_ref[rows, :] = dh1
            gb = dh1.astype(BF16)
            gb_ref[rows, :] = gb
            gbt_ref[:, rows] = gb.T
            sums_ref[5:6, :] += jnp.sum(gb.astype(F32), 0, keepdims=True)


def attention_backward(
    x_ref, g_ref, rows_ref, dh1_ref, gb_ref, gbt_ref, q_ref, v_ref, kt_ref, p_ref,
    o_ref, a1t_ref,
    d0_ref, xg_ref, sums_ref, bqv_ref,
    do_ref, delta_ref, dqt_ref, dq_ref, dk_ref, dv_ref, da1_ref,
):
    t = pl.program_id(0)
    n = x_ref.shape[0]
    width = g_ref.shape[-1]
    heads = width // HEAD_DIM
    step = 256
    pick = (
        lax.broadcasted_iota(jnp.int32, (16, width), 1) // HEAD_DIM
        == lax.broadcasted_iota(jnp.int32, (16, width), 0)
    ).astype(BF16)

    @pl.loop(0, n // step)
    def _(b):
        rows = pl.ds(pl.multiple_of(b * step, step), step)
        do = dot_nn(gb_ref[rows, :], g_ref[0, 3]).astype(BF16)
        do_ref[rows, :] = do
        prod = do.astype(F32) * o_ref[0, rows, :].astype(F32)
        high = prod.astype(BF16)
        low = (prod - high.astype(F32)).astype(BF16)
        delta_ref[:, rows] = dot_nt(pick, high) + dot_nt(pick, low)

    dqt_ref[...] = jnp.zeros_like(dqt_ref)
    for b in range(n // step):
        first, last = b * step, (b + 1) * step
        do = do_ref[first:, :]
        q = q_ref[0, first:, :]
        v = v_ref[0, first:last, :]
        dk, dv = None, None
        for h in range(heads):
            mine = head_mask((1, width), h)
            zero = jnp.zeros((), BF16)
            p = p_ref[0, h, first:last, first:]
            dp = dot_nt(jnp.where(mine, v, zero), do)
            ds = (p.astype(F32) * (dp - delta_ref[h : h + 1, first:])).astype(BF16)
            part = dot_nn(p, jnp.where(mine, do, zero))
            dv = part if dv is None else dv + part
            part = dot_nn(ds, jnp.where(mine, q, zero))
            dk = part if dk is None else dk + part
            head = slice(h * HEAD_DIM, (h + 1) * HEAD_DIM)
            dqt_ref[head, first:] += dot_nn(kt_ref[0, head, first:last], ds)
        dk_ref[first:last, :] = dk.astype(BF16)
        dv_ref[first:last, :] = dv.astype(BF16)

    @pl.when(t == 0)
    def _():
        da1_ref[...] = jnp.zeros_like(da1_ref)

    bqv_ref[...] = jnp.zeros_like(bqv_ref)

    @pl.loop(0, n // step)
    def _(b):
        rows = pl.ds(pl.multiple_of(b * step, step), step)
        dq = (dqt_ref[:, rows] * HEAD_DIM ** -0.5).astype(BF16).T
        dk = dk_ref[rows, :]
        dv = dv_ref[rows, :]
        dq_ref[rows, :] = dq
        bqv_ref[0, 0:1, :] += jnp.sum(dq.astype(F32), 0, keepdims=True)
        bqv_ref[0, 1:2, :] += jnp.sum(dv.astype(F32), 0, keepdims=True)
        da1_ref[rows, :] += (
            dot_nt(dq, g_ref[0, 0]) + dot_nt(dk, g_ref[0, 1]) + dot_nt(dv, g_ref[0, 2])
        )

    @pl.loop(0, D // step)
    def _(b):
        rows = pl.ds(pl.multiple_of(b * step, step), step)
        a1t = a1t_ref[rows, :]
        d0_ref[0, 0, rows, :] = dot_nn(a1t, dq_ref[...]).astype(BF16)
        d0_ref[0, 1, rows, :] = dot_nn(a1t, dk_ref[...]).astype(BF16)
        d0_ref[0, 2, rows, :] = dot_nn(a1t, dv_ref[...]).astype(BF16)
        d0_ref[0, 3, rows, :] = dot_nn(gbt_ref[rows, :], o_ref[0]).astype(BF16)

    @pl.when(t == pl.num_programs(0) - 1)
    def _():
        sums_ref[...] = jnp.zeros_like(sums_ref)

        @pl.loop(0, n // step)
        def _(b):
            rows = pl.ds(pl.multiple_of(b * step, step), step)
            xhat, r = norm_parts(x_ref[rows, :].astype(F32))
            da1 = da1_ref[rows, :]
            sums_ref[0:1, :] += jnp.sum(da1 * xhat, 0, keepdims=True)
            sums_ref[1:2, :] += jnp.sum(da1, 0, keepdims=True)
            dg = da1 * rows_ref[0:1, :]
            dv = r * (
                dg
                - jnp.mean(dg, -1, keepdims=True)
                - xhat * jnp.mean(dg * xhat, -1, keepdims=True)
            )
            xg_ref[rows, :] = (dh1_ref[rows, :] + dv).astype(BF16)


def whole(*shape):
    return pl.BlockSpec(shape, lambda t: (0,) * len(shape))


def group(*shape):
    return pl.BlockSpec((1,) + shape, lambda t: (t,) + (0,) * len(shape))


def shaped(dtype, *shape):
    return jax.ShapeDtypeStruct(shape, dtype)


SMEM_WHOLE = pl.BlockSpec(memory_space=pltpu.SMEM)


def run_attention_forward(length, x, g0, rows, bqv):
    n = x.shape[0]
    groups, _, _, width = g0.shape
    heads = width // HEAD_DIM
    return pl.pallas_call(
        attention_forward,
        grid=(groups,),
        in_specs=[SMEM_WHOLE, whole(n, D), group(4, D, width), whole(16, D), group(2, width)],
        out_specs=[
            group(n, width), group(n, width), group(width, n), group(heads, n, n),
            group(n, width), whole(D, n), whole(n, D), whole(n, D), whole(D, n),
        ],
        out_shape=[
            shaped(BF16, groups, n, width), shaped(BF16, groups, n, width),
            shaped(BF16, groups, width, n), shaped(BF16, groups, heads, n, n),
            shaped(BF16, groups, n, width), shaped(BF16, D, n), shaped(F32, n, D),
            shaped(BF16, n, D), shaped(BF16, D, n),
        ],
        scratch_shapes=[
            pltpu.VMEM((n, D), BF16), pltpu.VMEM((n, width), BF16),
            pltpu.VMEM((width, n), BF16), pltpu.VMEM((width, n), BF16),
            pltpu.VMEM((n, D), F32),
        ],
        compiler_params=pltpu.CompilerParams(vmem_limit_bytes=VMEM_LIMIT),
        name="attention_forward",
    )(length, x, g0, rows, bqv)


def run_feed_forward(length, cot, a2, a2t, h1, g1, g2, rows):
    n = cot.shape[0]
    groups, _, width = g1.shape
    return pl.pallas_call(
        feed_forward_both,
        grid=(groups,),
        in_specs=[
            SMEM_WHOLE, whole(n, D), whole(n, D), whole(D, n), whole(n, D),
            group(D, width), group(D, width), whole(16, D),
        ],
        out_specs=[
            whole(n, D), group(D, width), group(D, width), whole(n, D), whole(n, D),
            whole(D, n), whole(16, D),
        ],
        out_shape=[
            shaped(BF16, n, D), shaped(BF16, groups, D, width), shaped(BF16, groups, D, width),
            shaped(F32, n, D), shaped(BF16, n, D), shaped(BF16, D, n), shaped(F32, 16, D),
        ],
        scratch_shapes=[
            pltpu.VMEM((n, D), BF16), pltpu.VMEM((D, n), BF16), pltpu.VMEM((n, D), F32),
            pltpu.VMEM((n, D), F32), pltpu.VMEM((n, width), BF16), pltpu.VMEM((n, width), BF16),
        ],
        compiler_params=pltpu.CompilerParams(vmem_limit_bytes=VMEM_LIMIT),
        name="feed_forward_both",
    )(length, cot, a2, a2t, h1, g1, g2, rows)


def run_attention_backward(x, g0, rows, dh1, gb, gbt, q, v, kt, p, o, a1t):
    n = x.shape[0]
    groups, _, _, width = g0.shape
    heads = width // HEAD_DIM
    return pl.pallas_call(
        attention_backward,
        grid=(groups,),
        in_specs=[
            whole(n, D), group(4, D, width), whole(16, D), whole(n, D), whole(n, D),
            whole(D, n), group(n, width), group(n, width), group(width, n),
            group(heads, n, n), group(n, width), whole(D, n),
        ],
        out_specs=[group(4, D, width), whole(n, D), whole(8, D), group(8, width)],
        out_shape=[
            shaped(BF16, groups, 4, D, width), shaped(BF16, n, D), shaped(F32, 8, D),
            shaped(F32, groups, 8, width),
        ],
        scratch_shapes=[
            pltpu.VMEM((n, width), BF16), pltpu.VMEM((16, n), F32), pltpu.VMEM((width, n), F32),
            pltpu.VMEM((n, width), BF16), pltpu.VMEM((n, width), BF16),
            pltpu.VMEM((n, width), BF16), pltpu.VMEM((n, D), F32),
        ],
        compiler_params=pltpu.CompilerParams(vmem_limit_bytes=VMEM_LIMIT),
        name="attention_backward",
    )(x, g0, rows, dh1, gb, gbt, q, v, kt, p, o, a1t)


Z_DEV, Y_DEV, X_DEV, C_DEV = 4, 2, 2, 2


class Place:
    def __init__(self):
        dp, self.t = lax.axis_index("dp"), lax.axis_index("tensor")
        self.dp = dp
        self.z, self.y = dp // 2, dp % 2
        self.x, self.c = self.t // 2, self.t % 2
        self.other_y = 1 - self.y
        self.zs = [
            self.z,
            self.z + 1 - 2 * (self.z % 2),
            self.z + 2 - 4 * (self.z // 2),
            3 - self.z,
        ]
        self.ts = [
            self.t,
            self.t + 1 - 2 * (self.t % 2),
            self.t + 2 - 4 * (self.t // 2),
            3 - self.t,
        ]
        self.to_z = [dict(dp=z * 2 + self.y) for z in self.zs]
        self.to_y = dict(dp=self.z * 2 + self.other_y)
        self.to_x = dict(tensor=self.ts[2])
        self.same_t = self.to_z[1:] + [dict(dp=z * 2 + self.other_y) for z in self.zs]
        self.same_dp = [dict(tensor=t) for t in self.ts[1:]]
        self.to_core = dict(tensor=self.ts[1])

    def group(self, k):
        return lax.select(
            k == 0, self.ts[0],
            lax.select(k == 1, self.ts[1], lax.select(k == 2, self.ts[2], self.ts[3])),
        )

    def greet(self, others=None):
        barrier = pltpu.get_barrier_semaphore()
        others = others or self.to_z[1:] + [self.to_y, self.to_x, self.to_core]
        for device in others:
            pl.semaphore_signal(
                barrier, inc=1, device_id=device, device_id_type=pl.DeviceIdType.MESH
            )
        pl.semaphore_wait(barrier, len(others))


class Pieces:
    def __init__(self, whole, pieces):
        self.whole, self.pieces = whole, pieces

    def start(self):
        for piece in self.pieces:
            piece.start()

    def wait_recv(self):
        self.whole.wait_recv()

    def wait_send(self):
        self.whole.wait_send()


class Links:
    def __init__(self, send_sem, recv_sem):
        self.send_sem, self.recv_sem = send_sem, recv_sem
        self.copies = []

    def add(self, device, src, dst, parts=1, axis=0):
        number = len(self.copies)

        def make(src, dst):
            return pltpu.make_async_remote_copy(
                src_ref=src,
                dst_ref=dst,
                send_sem=self.send_sem.at[number],
                recv_sem=self.recv_sem.at[number],
                device_id=device,
                device_id_type=pl.DeviceIdType.MESH,
            )

        size = src.shape[axis] // parts
        cuts = [(slice(None),) * axis + (pl.ds(i * size, size),) for i in range(parts)]
        copy = Pieces(make(src, dst), [make(src.at[cut], dst.at[cut]) for cut in cuts])
        self.copies.append(copy)
        return copy

    def sent(self, *apart):
        for copy in self.copies:
            if all(copy is not other for other in apart):
                copy.wait_send()


def flat(copies):
    for item in copies:
        if isinstance(item, list):
            yield from flat(item)
        else:
            yield item


def start(*copies):
    for copy in flat(copies):
        copy.start()


def recv(*copies):
    for copy in flat(copies):
        copy.wait_recv()


class Gather:
    def __init__(self, links, place, own, full, order, single=True, last=True):
        every = slice(None)
        y, other = place.y, place.other_y

        def same(device, k, yy, to):
            return links.add(device, full(k, every, yy), full(to, every, yy), Z_DEV)

        def along_z(k, yy, block):
            here, passed = full(k, place.z, yy), full(k, place.zs[2], yy)
            return [
                links.add(place.to_z[1], block, here),
                links.add(place.to_z[2], block, here),
                links.add(place.to_z[1], passed, passed),
            ]

        if order != WHOLE:
            self.z = along_z(0, y, own)
        if order == X_Z_Y:
            self.first = [links.add(place.to_x, own, full(2, place.z, y), 2)]
            self.far = along_z(2, y, full(2, place.z, y))
            blocks = [(0, y), (2, y), (0, other), (2, other)]
        else:
            blocks = [(0, y), (0, other), (2, y), (2, other)]
        if order == Y_Z_X:
            self.first = [links.add(place.to_y, own, full(0, place.z, y), 2)]
            self.far = along_z(0, other, full(0, place.z, other))
        if order == Z_Y_X and single:
            self.first = [same(place.to_y, 0, y, 0)]
        if order == Z_Y_X and not single:
            self.first = [links.add(place.to_y, own, full(0, place.z, y))]
            for k in range(1, 4):
                block = full(0, place.zs[k], y)
                self.first.append(links.add(place.to_y, block, block))
            return
        self.second = [
            same(place.to_y, k, yy, k) if order == X_Z_Y else same(place.to_x, k, yy, 2)
            for k, yy in blocks[: 2 if last else 1]
        ]
        if not last:
            blocks = [block for block in blocks if block[0] == 0]
        self.core = [same(place.to_core, k, yy, k + 1) for k, yy in blocks]


Z_Y_X, Y_Z_X, X_Z_Y, WHOLE = range(4)


def fused_forward(
    tie_ref, len_ref, tokens_ref, gains_ref, bias_ref, in_ref, out_ref, expand_ref,
    project_ref,
    gq_ref, gw_ref, flat1_ref, flat2_ref, rows_ref,
    q_ref, v_ref, kt_ref, p_ref, scale_ref, o_ref, a1t_out, h1_out, a2_out, a2t_out,
    own0_ref, own1_ref, own2_ref, square_ref, vec_ref,
    all0_ref, w1_ref, w2_ref, vecs_ref, bqv_ref, x_ref, a1_ref, k_ref, qa_ref, vt_ref, ot_ref, a1t_ref, h1_ref, a2_ref, a2t_ref,
    send_sem, recv_sem, local_sem, flush_sem, row_sem,
):
    t, h = pl.program_id(0), pl.program_id(1)
    n, _ = x_ref.shape
    width = q_ref.shape[-1]
    heads = width // HEAD_DIM
    step = 256
    place = Place()
    length = len_ref[place.t]
    links = Links(send_sem, recv_sem)
    z, y, x, c = place.z, place.y, place.x, place.c
    mine_there = vecs_ref.at[z, y, x, c]
    column = vecs_ref.at[:, :, x, c]
    vec_one = [links.add(device, vec_ref, mine_there) for device in place.same_t]
    vec_two = [links.add(device, column, column) for device in place.same_dp]
    half = own0_ref.shape[0] // 2
    halves = []
    for i in range(2):
        rows = pl.ds(i * half, half)
        halves.append(Gather(
            links, place, own0_ref.at[rows],
            lambda k, z, y, rows=rows: all0_ref.at[k, z, y, rows], Z_Y_X, single=False,
        ))
    seg0 = Gather(links, place, own0_ref, lambda k, z, y: all0_ref.at[k, z, y], WHOLE)
    seg1 = Gather(
        links, place, own1_ref, lambda k, z, y: w1_ref.at[k, z, y], Y_Z_X, last=False
    )
    seg2 = Gather(
        links, place, own2_ref, lambda k, z, y: w2_ref.at[k, z, y], X_Z_Y, last=False
    )
    flush = [
        [
            pltpu.make_async_copy(ref.at[k], flat.at[k], flush_sem.at[i, k])
            for k in range(3)
        ]
        for i, (ref, flat) in enumerate([(w1_ref, flat1_ref), (w2_ref, flat2_ref)])
    ]
    put_a1t = pltpu.make_async_copy(a1t_ref, a1t_out, local_sem.at[0])
    put_a2t = pltpu.make_async_copy(a2t_ref, a2t_out, local_sem.at[1])
    puts = []
    for i in range(n // step):
        rows = pl.ds(i * step, step)
        puts.append([
            pltpu.make_async_copy(h1_ref.at[rows], h1_out.at[rows], row_sem.at[0, i]),
            pltpu.make_async_copy(a2_ref.at[rows], a2_out.at[rows], row_sem.at[1, i]),
        ])
    fetch = pltpu.make_async_copy(tokens_ref.at[place.t], x_ref, local_sem.at[2])

    def relay_z(copies):
        recv(copies[1])
        start(copies[2])

    def pass_own(seg):
        recv(seg.z[0], seg.z[2])
        start(seg.second[0], seg.core[0])

    def pass_second(seg):
        recv(seg.second)
        if seg is seg2:
            start(seg.core[1])

    def pass_first(seg):
        recv(seg.first)
        start(seg.far[1], seg.far[0])

    def pass_far(seg):
        recv(seg.far[0], seg.far[2])
        start(seg.core[1:] if seg is seg1 else [])

    def pass_core(seg, i):
        recv(seg.second[i])
        start(seg.core[2 + i])

    plan = [
        (0, 0, lambda: (pass_first(seg1), relay_z(seg2.z), pass_first(seg2))),
        (0, 3, lambda: (relay_z(seg1.z), pass_core(seg0, 0))),
        (1, 0, lambda: recv(seg0.core[:2])),
        (1, 1, lambda: relay_z(seg1.far)),
        (1, 3, lambda: pass_core(seg0, 1)),
        (1, 4, lambda: pass_own(seg2)),
        (2, 1, lambda: relay_z(seg2.far)),
        (2, 3, lambda: pass_own(seg1)),
        (3, 0, lambda: (recv(seg0.core[2:]), pass_far(seg1), flush[0][0].start())),
        (3, 2, lambda: (pass_second(seg2), flush[1][0].start())),
        (3, 3, lambda: (pass_far(seg2), flush[1][2].start())),
    ]

    def serve(points):
        for step, where, act in plan:
            if where in points:
                now = (t == step) & (h == max(where - 2, 0))
                pl.when(now)(lambda act=act: (act(), None)[1])

    @pl.when((t == 0) & (h == 0))
    def _():
        s0, s1, s2, s3 = tie_ref[0], tie_ref[1], tie_ref[2], tie_ref[3]
        fetch.start()
        square_ref[...] = jnp.zeros_like(square_ref)
        gain = gains_ref.shape[-1]
        square_ref[0:1, :gain] = gains_ref[s0].astype(F32)[0:1]
        square_ref[1:2, :gain] = gains_ref[s2].astype(F32)[1:2]
        kinds = [s0, s0, s0, s1, s2, s3, s2, s2, s2, s2]
        for i, source in enumerate(kinds):
            wide = bias_ref[i].astype(F32)
            here = lax.broadcasted_iota(jnp.int32, wide.shape, 0) == source
            square_ref[2 + i : 3 + i, :gain] = jnp.sum(
                jnp.where(here, wide, 0.0), 0, keepdims=True
            )
        vec_ref[...] = square_ref[...].T[:gain]
        for j in range(3):
            own0_ref[:, j * width : (j + 1) * width] = in_ref[s0, j]
        own0_ref[:, 3 * width :] = out_ref[s1].T
        place.greet(place.same_t + place.same_dp)
        start(vec_one)
        for part in halves:
            start(part.z[1], part.z[0], part.first[0])
        vecs_ref[z, y, x, c] = vec_ref[...]
        ones = lax.broadcasted_iota(jnp.int32, (vt_ref.shape[1] - HEAD_DIM, n), 0) == 0
        for h in range(heads):
            vt_ref[h, HEAD_DIM:, :] = ones.astype(BF16)
        all0_ref[0, z, y] = own0_ref[...]
        own1_ref[...] = expand_ref[s2]
        own2_ref[...] = project_ref[s3]
        w1_ref[0, z, y] = own1_ref[...]
        w2_ref[0, z, y] = own2_ref[...]
        recv(vec_one)
        start(vec_two)
        for part in halves:
            relay_z(part.z)
            start(part.first[2])
        for part in halves:
            recv(part.z[0])
            start(part.first[1])
        start(seg2.z[1])
        recv(vec_two)
        start(seg2.first)
        vecs = vecs_ref[...].reshape(D, vecs_ref.shape[-1]).T[:16]
        rows_ref[...] = vecs
        for part in halves:
            recv(part.z[2])
            start(part.first[3])
        start(seg1.first, seg0.second[0], seg0.core[0])
        for k in range(4):
            part = slice(k * width, (k + 1) * width)
            bqv_ref[k, 0:1, :width] = vecs[3:4, part]
            bqv_ref[k, 0:1, width : 2 * width] = jnp.zeros((1, width), F32)
            bqv_ref[k, 0:1, 2 * width :] = vecs[4:5, part]
        fetch.wait()

        @pl.loop(0, n // step)
        def _(b):
            rows = pl.ds(pl.multiple_of(b * step, step), step)
            wide = x_ref[rows, :].astype(F32)
            xhat, _ = norm_parts(wide)
            a1 = (xhat * rows_ref[0:1, :] + rows_ref[2:3, :]).astype(BF16)
            a1_ref[rows, :] = a1
            a1t_ref[:, rows] = a1.T
            h1_ref[rows, :] = wide + rows_ref[5:6, :]

        put_a1t.start()
        start(seg2.z[0], seg1.z[1], seg1.z[0])
        recv(halves[0].first, halves[1].first)
        start(seg0.second[1], seg0.core[1])

    serve([0])

    @pl.when(h == 0)
    def _():
        here = all0_ref[t].reshape(D, 4 * width)
        gq = here[:, : 3 * width]
        gq_ref[0] = gq
        gw_ref[0] = here[:, 3 * width :]
        mine = place.group(t)
        qkv = dot_nn(a1_ref[...], gq) + bqv_ref[mine, 0:1, :]
        q = qkv[:, :width].astype(BF16) * jnp.asarray(HEAD_DIM ** -0.5, BF16)
        k = qkv[:, width : 2 * width].astype(BF16)
        v = qkv[:, 2 * width :].astype(BF16)
        q_ref[0] = q
        kt_ref[0] = k.T
        v_ref[0] = v
        vt = v.T
        for h in range(heads):
            vt_ref[h, :HEAD_DIM, :] = vt[h * HEAD_DIM : (h + 1) * HEAD_DIM]
        spare = k_ref.shape[1] - width
        dead = lax.broadcasted_iota(jnp.int32, (n, spare), 0) >= length
        first_column = lax.broadcasted_iota(jnp.int32, (n, spare), 1) == 0
        k_ref[:, :width] = k
        k_ref[:, width:] = jnp.where(first_column & dead, MASKED, 0.0).astype(BF16)
        qa_ref[:, :width] = q
        qa_ref[:, width:] = jnp.where(first_column, 1.0, 0.0).astype(BF16)
        scale_ref[0, heads:, :] = jnp.zeros((scale_ref.shape[1] - heads, n), F32)

    serve([1])

    lane = lax.broadcasted_iota(jnp.int32, (1, qa_ref.shape[1]), 1)
    keep = ((lane >= h * HEAD_DIM) & (lane < (h + 1) * HEAD_DIM)) | (lane >= width)
    key = lax.broadcasted_iota(jnp.int32, (step, step), 0)
    query = lax.broadcasted_iota(jnp.int32, (step, step), 1)
    head = pl.ds(pl.multiple_of(h * HEAD_DIM, HEAD_DIM), HEAD_DIM)

    def scores(b):
        first, last = b * step, (b + 1) * step
        q = jnp.where(keep, qa_ref[first:last, :], jnp.zeros((), BF16))
        return dot_nt(k_ref[:last, :], q)

    def attend(b, s):
        first, last = b * step, (b + 1) * step
        near = jnp.where(key <= query, s[first:], MASKED)
        top = jnp.max(near, 0, keepdims=True)
        if b:
            far = s[:first]
            top = jnp.maximum(top, jnp.max(far, 0, keepdims=True))
        e_near = jnp.exp((near - top).astype(BF16))
        p_ref[0, 0, b, first:last, :] = e_near
        o = dot_nn(vt_ref[h, :, first:last], e_near)
        if b:
            e_far = jnp.exp((far - top).astype(BF16))
            p_ref[0, 0, b, :first, :] = e_far
            o += dot_nn(vt_ref[h, :, :first], e_far)
        scale = 1.0 / o[HEAD_DIM : HEAD_DIM + 1]
        scale_ref[0, pl.ds(h, 1), first:last] = scale
        ot_ref[head, first:last] = (o[:HEAD_DIM] * scale).astype(BF16)

    s = scores(0)
    for b in range(n // step):
        ahead = scores(b + 1) if b + 1 < n // step else None
        attend(b, s)
        s = ahead

    serve([2, 3, 4])

    @pl.when(h == heads - 1)
    def _():
        o = ot_ref[...].T
        o_ref[0] = o
        h1_ref[...] += dot_nt(o, gw_ref[0])

    @pl.when((t == 3) & (h == heads - 1))
    def _():
        for i, rows in enumerate(blocks(n, step)):
            xhat, _ = norm_parts(h1_ref[rows, :])
            a2 = (xhat * rows_ref[1:2, :] + rows_ref[6:7, :]).astype(BF16)
            a2_ref[rows, :] = a2
            a2t_ref[:, rows] = a2.T
            for put in puts[i]:
                put.start()
        put_a2t.start()
        recv(seg2.core)
        flush[1][1].start()
        recv(seg1.core)
        flush[0][1].start()
        pass_second(seg1)
        flush[0][2].start()
        links.sent()
        for copies in flush + puts + [[put_a1t, put_a2t]]:
            for copy in copies:
                copy.wait()


N_GATHER = 10 + 14 + 6 + 10 + 10
VMEM_WHOLE = pl.BlockSpec(memory_space=pltpu.VMEM)
ANY_WHOLE = pl.BlockSpec(memory_space=pl.ANY)


def run_fused_forward(tie, lengths, tokens, gains, biases, w_in, w_out, w_expand, w_project):
    groups, n, _ = tokens.shape
    depth, width = w_in.shape[-2:]
    heads = width // HEAD_DIM
    hidden = w_expand.shape[-1]
    w_project = w_project.transpose(0, 2, 1)
    biases = biases.transpose(1, 0, 2)
    own = gains.shape[-1]

    def group(*shape):
        return pl.BlockSpec((1,) + shape, lambda t, h: (t,) + (0,) * len(shape))

    per_head = pl.BlockSpec((1, 1, n // 256, n, 256), lambda t, h: (t, h, 0, 0, 0))
    return pl.pallas_call(
        fused_forward,
        grid=(groups, heads),
        in_specs=[SMEM_WHOLE, SMEM_WHOLE, ANY_WHOLE] + [VMEM_WHOLE] * 6,
        out_specs=[
            group(D, 3 * width), group(D, width), ANY_WHOLE, ANY_WHOLE, VMEM_WHOLE,
            group(n, width), group(n, width), group(width, n), per_head,
            group(8, n), group(n, width), ANY_WHOLE, ANY_WHOLE, ANY_WHOLE, ANY_WHOLE,
        ],
        out_shape=[
            shaped(BF16, groups, D, 3 * width), shaped(BF16, groups, D, width),
            shaped(BF16, groups, Z_DEV, Y_DEV, depth, hidden),
            shaped(BF16, groups, Z_DEV, Y_DEV, depth, hidden),
            shaped(F32, 16, D),
            shaped(BF16, groups, n, width), shaped(BF16, groups, n, width),
            shaped(BF16, groups, width, n), shaped(BF16, groups, heads, n // 256, n, 256),
            shaped(F32, groups, 8, n), shaped(BF16, groups, n, width), shaped(BF16, D, n), shaped(F32, n, D),
            shaped(BF16, n, D), shaped(BF16, D, n),
        ],
        scratch_shapes=[
            pltpu.VMEM((depth, 4 * width), BF16),
            pltpu.VMEM((depth, hidden), BF16), pltpu.VMEM((depth, hidden), BF16),
            pltpu.VMEM((128, 128), F32), pltpu.VMEM((own, 128), F32),
            pltpu.VMEM((groups, Z_DEV, Y_DEV, depth, 4 * width), BF16),
            pltpu.VMEM((groups, Z_DEV, Y_DEV, depth, hidden), BF16),
            pltpu.VMEM((groups, Z_DEV, Y_DEV, depth, hidden), BF16),
            pltpu.VMEM((Z_DEV, Y_DEV, X_DEV, C_DEV, own, 128), F32),
            pltpu.VMEM((groups, 8, 3 * width), F32),
            pltpu.VMEM((n, D), BF16), pltpu.VMEM((n, D), BF16), pltpu.VMEM((n, 256), BF16),
            pltpu.VMEM((n, 256), BF16), pltpu.VMEM((heads, HEAD_DIM + 16, n), BF16),
            pltpu.VMEM((width, n), BF16),
            pltpu.VMEM((D, n), BF16), pltpu.VMEM((n, D), F32), pltpu.VMEM((n, D), BF16),
            pltpu.VMEM((D, n), BF16),
            pltpu.SemaphoreType.DMA((N_GATHER,)), pltpu.SemaphoreType.DMA((N_GATHER,)),
            pltpu.SemaphoreType.DMA((3,)), pltpu.SemaphoreType.DMA((2, 4)),
            pltpu.SemaphoreType.DMA((2, n // 256)),
        ],
        compiler_params=pltpu.CompilerParams(
            vmem_limit_bytes=VMEM_LIMIT, collective_id=0, has_side_effects=True
        ),
        name="fused_forward",
    )(tie, lengths, tokens, gains, biases, w_in, w_out, w_expand, w_project)


class Result:
    def __init__(self, links, place, own_ref, passing_ref, out_ref, step, sem, count):
        self.x, self.core, self.far, self.keep, self.keep_far = [], [], [], [], []
        for i in range(count):
            rows = pl.ds(i * step, step)
            mine, theirs = out_ref.at[place.t, rows], out_ref.at[place.ts[2], rows]
            own, passing = own_ref.at[rows], passing_ref.at[rows]
            self.x.append(links.add(place.to_x, own, passing))
            self.core.append(links.add(place.to_core, own, mine))
            self.far.append(links.add(place.to_core, passing, theirs))
            self.keep.append(pltpu.make_async_copy(own, mine, sem.at[0, i]))
            self.keep_far.append(pltpu.make_async_copy(passing, theirs, sem.at[1, i]))

    def send(self, i):
        start(self.x[i], self.core[i], self.keep[i])

    def pass_on(self, i):
        recv(self.x[i])
        start(self.far[i], self.keep_far[i])

    def finish(self):
        recv(self.core, self.far)
        for copy in self.keep + self.keep_far:
            copy.wait()


def low(value):
    return jnp.asarray(value, BF16)


def pair_order(i):
    return i + 1 - 2 * (i % 2)


def fused_feed_forward(
    len_ref, cot_ref, a2_ref, a2t_in, h1_in, far1_ref, far2_ref, rows_ref,
    out_out, fold_ref, work_out, dh1_out, gb_out, gbt_out, sums_ref,
    gf_ref, gft_ref, feed_ref, da2_ref, h_ref, df_ref, weights_ref, missing_ref, third_ref,
    stage_ref, land_ref, near_ref, cross_ref, a2t_ref, h1_ref, out_ref, work_ref,
    send_sem, recv_sem, local_sem, row_sem,
):
    t = pl.program_id(0)
    n = gf_ref.shape[0]
    step = 256
    depth = stage_ref.shape[-2]
    place = Place()
    length = len_ref[place.t]
    links = Links(send_sem, recv_sem)
    y, other = place.y, place.other_y
    last = [
        links.add(place.to_x, far1_ref.at[0, :, other], missing_ref.at[0, 0]),
        links.add(place.to_y, far2_ref.at[2, :, y], missing_ref.at[1, 0]),
    ]
    last_core = [
        links.add(place.to_core, missing_ref.at[i, 0], missing_ref.at[i, 1]) for i in range(2)
    ]
    third = [
        links.add(place.to_core, far_ref.at[2, :, y], third_ref.at[i])
        for i, far_ref in enumerate([far1_ref, far2_ref])
    ]
    core = [
        [links.add(place.to_core, stage_ref.at[i], land_ref.at[s, i]) for i in range(2)]
        for s in range(2)
    ]
    cross = [
        links.add(place.to_y, near_ref.at[i, :, other], cross_ref.at[i]) for i in range(2)
    ]
    fetch = pltpu.make_async_copy(cot_ref.at[place.t], gf_ref, local_sem.at[0])
    gb_ref, gbt_ref, dh1_ref = gf_ref, gft_ref, da2_ref
    late = [
        pltpu.make_async_copy(a2t_in, a2t_ref, local_sem.at[5]),
        pltpu.make_async_copy(h1_in, h1_ref, local_sem.at[6]),
    ]
    puts = []
    for i in range(n // step):
        rows = pl.ds(i * step, step)
        puts.append([
            pltpu.make_async_copy(ref.at[rows], out.at[rows], row_sem.at[j, i])
            for j, (ref, out) in enumerate(
                [(out_ref, out_out), (dh1_ref, dh1_out), (gb_ref, gb_out)]
            )
        ])
    put_gbt = pltpu.make_async_copy(gbt_ref, gbt_out, local_sem.at[7])
    put_work = pltpu.make_async_copy(work_ref, work_out, local_sem.at[8])
    k = pair_order(t)
    mine = place.group(k)

    def load(step, whole, slot):
        for i, far_ref in enumerate([far1_ref, far2_ref]):
            group = far_ref.at[pair_order(step)]
            to = weights_ref.at[slot, i]
            if not whole:
                group, to = group.at[:, y], to.at[:, y]
            yield pltpu.make_async_copy(group, to, local_sem.at[1 + 2 * slot + i])

    def live_rows(b):
        at = b * step + lax.broadcasted_iota(jnp.int32, (step, 1), 0)
        return (at < length).astype(F32)

    @pl.when(t == 0)
    def _():
        fetch.start()
        for copy in load(0, True, 0):
            copy.start()
        for copy in late:
            copy.start()
        place.greet()
        start(last, third)
        sums_ref[...] = jnp.zeros_like(sums_ref)
        feed_ref[...] = jnp.zeros_like(feed_ref)
        da2_ref[...] = jnp.zeros_like(da2_ref)
        fetch.wait()

        @pl.loop(0, n // step)
        def _(b):
            rows = pl.ds(pl.multiple_of(b * step, step), step)
            g = (gf_ref[rows, :].astype(F32) * live_rows(b)).astype(BF16)
            gf_ref[rows, :] = g
            gft_ref[:, rows] = g.T
            sums_ref[7:8, :] += jnp.sum(g.astype(F32), 0, keepdims=True)

    for i in range(4):
        @pl.when(t == i)
        def _():
            if i == 2:
                recv(last_core, third)
            else:
                for copy in load(i, i < 2, i % 2):
                    copy.wait()
            if i in (0, 2):
                for copy in load(i + 1, i + 1 < 2, (i + 1) % 2):
                    copy.start()
            for j in range(2):
                if i == 2:
                    weights_ref[0, j, :, y] = third_ref[j]
                if i >= 2:
                    weights_ref[i % 2, j, :, other] = missing_ref[j, 3 - i]

    bias = rows_ref[pl.ds(8 + mine, 1), :]
    w1 = weights_ref[t % 2, 0].reshape(D, -1)
    w2 = weights_ref[t % 2, 1].reshape(D, -1)
    column = jnp.zeros((1, w1.shape[1]), F32)
    for rows in blocks(n, step):
        f = (dot_nn(a2_ref[rows, :], w1) + bias).astype(BF16)
        dh = dot_nn(gf_ref[rows, :], w2)
        f2 = f * f
        th = jnp.tanh(f * (low(SQRT_2_PI) + low(SQRT_2_PI * 0.044715) * f2))
        half = low(0.5) + low(0.5) * th
        h = f * half
        slope = half + f * (low(0.5) - low(0.5) * th * th) * (
            low(SQRT_2_PI) + low(3 * SQRT_2_PI * 0.044715) * f2
        )
        df = (dh * slope.astype(F32)).astype(BF16)
        h_ref[rows, :] = h
        df_ref[rows, :] = df
        column += jnp.sum(df.astype(F32), 0, keepdims=True)
        feed_ref[rows, :] += dot_nt(h, w2)
        da2_ref[rows, :] += dot_nt(df, w1)
    sums_ref[pl.ds(8 + mine, 1), :] = column

    @pl.when(t == 1)
    def _():
        recv(last)
        start(last_core)

    @pl.when(t == 0)
    def _():
        late[0].wait()

    def weight_grad(left_ref, right_ref):
        value = dot_nn(left_ref[...], right_ref[...])
        return value.reshape(Z_DEV, Y_DEV, depth, value.shape[-1]).astype(BF16)

    grad1 = weight_grad(a2t_ref, df_ref)
    grad2 = weight_grad(gft_ref, h_ref)

    def put(ref):
        ref[0] = grad1
        ref[1] = grad2

    def reduced(ref):
        return lambda i, s, z: (
            ref[i, z].astype(F32) + land_ref[s, i, z].astype(F32)
        ).astype(BF16)

    @pl.when(t == 0)
    def _():
        put(stage_ref)
        start(core[0])

    @pl.when(t == 1)
    def _():
        put(near_ref)
        recv(core[0])

        @pl.loop(0, Z_DEV)
        def _(z):
            for i in range(2):
                near_ref[i, z] = reduced(near_ref)(i, 0, z)

        start(cross)

    @pl.when(t == 2)
    def _():
        for copy in core[0]:
            copy.wait_send()
        put(stage_ref)
        start(core[1])

    @pl.when(t == 3)
    def _():
        put(work_ref)
        late[1].wait()
        for i, rows in enumerate(blocks(n, step)):
            live = live_rows(i)
            h1 = h1_ref[rows, :]
            out_ref[rows, :] = (live * (h1 + (feed_ref[rows, :] + rows_ref[7:8, :]))).astype(BF16)
            xhat, r = norm_parts(h1)
            da2 = da2_ref[rows, :]
            sums_ref[1:2, :] += jnp.sum(da2 * xhat, 0, keepdims=True)
            sums_ref[6:7, :] += jnp.sum(da2, 0, keepdims=True)
            dg = da2 * rows_ref[1:2, :]
            dv = r * (
                dg
                - jnp.mean(dg, -1, keepdims=True)
                - xhat * jnp.mean(dg * xhat, -1, keepdims=True)
            )
            dh1 = gf_ref[rows, :].astype(F32) + dv
            dh1_ref[rows, :] = dh1
            gb = dh1.astype(BF16)
            gb_ref[rows, :] = gb
            gbt_ref[:, rows] = gb.T
            sums_ref[5:6, :] += jnp.sum(gb.astype(F32), 0, keepdims=True)
            for copy in puts[i]:
                copy.start()
        put_gbt.start()
        recv(core[1])

        @pl.loop(0, Z_DEV)
        def _(z):
            for i in range(2):
                work_ref[i, z] = reduced(work_ref)(i, 1, z)

        put_work.start()
        recv(cross)

        @pl.loop(0, Z_DEV)
        def _(z):
            for i in range(2):
                fold_ref[i, z] = (
                    near_ref[i, z, y].astype(F32) + cross_ref[i, z].astype(F32)
                ).astype(BF16)

        links.sent(*core[0])
        for copies in puts + [[put_gbt, put_work]]:
            for copy in copies:
                copy.wait()


def run_fused_feed_forward(lengths, cot, a2, a2t, h1, g1, g2, rows):
    n = cot.shape[1]
    groups, _, _, depth, hidden = g1.shape
    both = (2, Z_DEV, Y_DEV, depth, hidden)
    fold = (2, Z_DEV, depth, hidden)
    return pl.pallas_call(
        fused_feed_forward,
        grid=(groups,),
        in_specs=[SMEM_WHOLE, ANY_WHOLE, VMEM_WHOLE] + [ANY_WHOLE] * 4 + [VMEM_WHOLE],
        out_specs=[ANY_WHOLE, VMEM_WHOLE] + [ANY_WHOLE] * 4 + [VMEM_WHOLE],
        out_shape=[
            shaped(BF16, n, D), shaped(BF16, *fold), shaped(BF16, *both), shaped(F32, n, D),
            shaped(BF16, n, D), shaped(BF16, D, n), shaped(F32, 16, D),
        ],
        scratch_shapes=[
            pltpu.VMEM((n, D), BF16), pltpu.VMEM((D, n), BF16), pltpu.VMEM((n, D), F32),
            pltpu.VMEM((n, D), F32), pltpu.VMEM((n, hidden), BF16), pltpu.VMEM((n, hidden), BF16),
            pltpu.VMEM((2,) + both, BF16),
            pltpu.VMEM((2,) + fold, BF16), pltpu.VMEM(fold, BF16), pltpu.VMEM(both, BF16),
            pltpu.VMEM((2,) + both, BF16),
            pltpu.VMEM(both, BF16), pltpu.VMEM(fold, BF16),
            pltpu.VMEM((D, n), BF16), pltpu.VMEM((n, D), F32), pltpu.VMEM((n, D), BF16),
            pltpu.VMEM(both, BF16),
            pltpu.SemaphoreType.DMA((12,)), pltpu.SemaphoreType.DMA((12,)),
            pltpu.SemaphoreType.DMA((9,)), pltpu.SemaphoreType.DMA((3, n // 256)),
        ],
        compiler_params=pltpu.CompilerParams(
            vmem_limit_bytes=VMEM_LIMIT, collective_id=1, has_side_effects=True
        ),
        name="fused_feed_forward",
    )(lengths, cot, a2, a2t, h1, g1, g2, rows)
class Reduce:
    def __init__(
        self, links, place, work, acc, cross_ref, far_ref, mid_ref, last_ref, side_ref,
        slots=(0, 1),
    ):
        self.place, self.work, self.acc = place, work, acc
        self.cross_ref, self.far_ref, self.mid_ref = cross_ref, far_ref, mid_ref
        self.last_ref, self.side_ref = last_ref, side_ref
        self.two = len(slots) == 2
        zs = place.zs
        self.y = {
            s: [
                links.add(
                    place.to_y, work(s, zs[j], place.other_y),
                    cross_ref.at[s if self.two else 0, zs[j]],
                )
                for j in (1, 3, 2, 0)
            ]
            for s in slots
        }
        self.z = [
            [
                links.add(place.to_z[1], acc(s, zs[1]), far_ref.at[s, 0]),
                links.add(place.to_z[1], acc(s, zs[3]), far_ref.at[s, 1]),
                links.add(place.to_z[2], mid_ref.at[s, 1], far_ref.at[s, 2]),
            ]
            for s in range(2)
        ]
        self.x = links.add(place.to_x, last_ref, side_ref)

    def fold_y(self, s, half):
        for i, j in [(0, 1), (1, 3), (2, 2), (3, 0)][2 * half : 2 * half + 2]:
            z = self.place.zs[j]
            recv(self.y[s][i])
            value = self.work(s, z, self.place.y)[...].astype(F32)
            cross = self.cross_ref[s if self.two else 0, z].astype(F32)
            self.acc(s, z)[...] = (value + cross).astype(BF16)
            if i < 2:
                start(self.z[s][i])

    def fold_z(self, s):
        recv(self.z[s][:2])
        for i in (1, 0):
            value = self.acc(s, self.place.zs[2 * i])[...].astype(F32)
            self.mid_ref[s, i] = (value + self.far_ref[s, i].astype(F32)).astype(BF16)
            if i:
                start(self.z[s][2])

    def own(self, s):
        recv(self.z[s][2])
        return self.mid_ref[s, 0].astype(F32) + self.far_ref[s, 2].astype(F32)

    def send_x(self):
        self.last_ref[...] = self.own(1).astype(BF16)
        start(self.x)

    def total(self):
        value = self.own(0)
        recv(self.x)
        return value + self.side_ref[...].astype(F32)


def fused_backward(
    tokens_ref, gq_in, gw_in, rows_ref, dh1_ref, gb_ref, gbt_in, q_in, v_in, kt_in,
    p_ref, scale_in, o_in, a1t_in, layer_in, fold_in, work_in, early_ref,
    out_ref, layerout_ref, part0_ref, part1_ref, part2_ref, total_ref,
    gq_ref, gw_ref, q_ref, v_ref, kt_ref, scale_ref, o_ref,
    a1t_ref, gbt_ref, layer_ref, fold_ref, work_ref, do_ref, delta_ref, dkv_ref, dqkv_ref, hold_ref, da1_ref, own_ref, passing_ref, passlayer_ref, bqv_ref,
    folded_ref, cross1_ref, far1_ref, mid1_ref, last1_ref, side1_ref,
    cross2_ref, far2_ref, mid2_ref, last2_ref, side2_ref,
    stage0_ref, land0_ref, work0_ref, cross0_ref, far0_ref, mid0_ref, last0_ref, side0_ref,
    sums_ref, sumland_ref,
    send_sem, recv_sem, local_sem, result_sem, group_sem,
):
    t = pl.program_id(0)
    n = own_ref.shape[0]
    width = gw_ref.shape[-1]
    depth = part0_ref.shape[0]
    heads = width // HEAD_DIM
    step = n // 4
    place = Place()
    y = place.y
    links = Links(send_sem, recv_sem)
    k, i = group_and_block(t)
    mine = place.group(k)
    now = k % 2
    out = Result(links, place, own_ref, passing_ref, out_ref, step, result_sem.at[0], 4)
    layer = Result(links, place, layer_ref, passlayer_ref, layerout_ref, step, result_sem.at[1], 4)
    fetch = pltpu.make_async_copy(tokens_ref.at[place.t], own_ref, local_sem.at[0])
    fetch_layer, fetch_work, fetch_fold, fetch_gbt, fetch_a1t = [
        pltpu.make_async_copy(there, here, local_sem.at[1 + j])
        for j, (there, here) in enumerate([
            (layer_in, layer_ref), (work_in, work_ref), (fold_in, fold_ref),
            (gbt_in, gbt_ref), (a1t_in, a1t_ref),
        ])
    ]
    def operands(group):
        slot = group % 2
        pairs = [
            (gw_in, gw_ref), (scale_in, scale_ref), (o_in, o_ref), (v_in, v_ref),
            (q_in, q_ref), (kt_in, kt_ref), (gq_in, gq_ref),
        ]
        return [
            pltpu.make_async_copy(there.at[group], here.at[slot], group_sem.at[slot, j])
            for j, (there, here) in enumerate(pairs)
        ]

    core0 = [links.add(place.to_core, stage0_ref, land0_ref.at[i]) for i in range(2)]
    def half_done(i, *landing):
        return Reduce(
            links, place, lambda s, z, y: work_ref.at[i, z, y],
            lambda s, z: folded_ref.at[i, z] if s else fold_ref.at[i, z],
            *landing, slots=(1,),
        )

    seg1 = half_done(0, cross1_ref, far1_ref, mid1_ref, last1_ref, side1_ref)
    seg2 = half_done(1, cross2_ref, far2_ref, mid2_ref, last2_ref, side2_ref)
    seg0 = Reduce(
        links, place, lambda s, z, y: work0_ref.at[s, z, y],
        lambda s, z: work0_ref.at[s, z, y],
        cross0_ref, far0_ref, mid0_ref, last0_ref, side0_ref,
    )
    sum_core, sum_y, *sum_z, sum_x = [
        links.add(to, sums_ref.at[i], sumland_ref.at[j])
        for j, (i, to) in enumerate(
            zip([0, 1, 2, 2, 2, 3], [place.to_core, place.to_y] + place.to_z[1:] + [place.to_x])
        )
    ]

    def when(point):
        return pl.when(t == point)

    @when(0)
    def _():
        start(fetch_layer, operands(1), fetch_work, fetch_fold, fetch_gbt, operands(0))
        start(fetch, fetch_a1t)
        place.greet()
        fetch_layer.wait()
        for i in range(4):
            layer.send(i)
        fetch_work.wait()
        start(seg1.y[1], seg2.y[1])
        fetch_fold.wait()
        start(seg1.z[0][:2], seg2.z[0][:2])
        bqv_ref[...] = jnp.zeros_like(bqv_ref)
        sums_ref[0] = early_ref[...]
        fetch_gbt.wait()

    def wait(copies):
        for copy in copies:
            copy.wait()

    @when(0)
    def _():
        wait(operands(1))

    @when(4)
    def _():
        start(operands(3))
        wait(operands(0))

    @when(8)
    def _():
        start(operands(2))
        wait(operands(3))

    @when(9)
    def _():
        wait(operands(2))

    plan = [
        (2, 1, lambda: (seg1.fold_y(1, 0), seg1.fold_z(0))),
        (3, 1, lambda: layer.pass_on(0)),
        (4, 0, lambda: (seg1.fold_y(1, 1), seg2.fold_z(0))),
        (4, 1, lambda: layer.pass_on(1)),
        (5, 1, lambda: (seg1.fold_z(1), seg2.fold_y(1, 0))),
        (8, 0, lambda: (seg2.fold_y(1, 1), layer.pass_on(2))),
        (8, 1, lambda: seg1.send_x()),
        (9, 1, lambda: (seg2.fold_z(1), seg0.fold_y(0, 0), layer.pass_on(3))),
        (11, 1, lambda: (seg2.send_x(), seg0.fold_y(0, 1))),
        (13, 1, lambda: (seg0.fold_z(0), out.pass_on(3))),
    ]

    def serve(point):
        for at, where, act in plan:
            if where == point:
                pl.when(t == at)(lambda act=act: (act(), None)[1])

    @pl.when((t == 0) | (t == 4) | (t == 8) | (t == 9))
    def _():
        pick = (
            lax.broadcasted_iota(jnp.int32, (8, width), 1) // HEAD_DIM
            == lax.broadcasted_iota(jnp.int32, (8, width), 0)
        ).astype(BF16)

        @pl.loop(0, n // step)
        def _(i):
            rows = pl.ds(pl.multiple_of(i * step, step), step)
            columns = scale_ref[now, :, rows].T
            lane = lax.broadcasted_iota(jnp.int32, (step, width), 1)
            scale = columns[:, heads - 1 : heads]
            for h in reversed(range(heads - 1)):
                scale = jnp.where(lane < (h + 1) * HEAD_DIM, columns[:, h : h + 1], scale)
            do = (dot_nn(gb_ref[rows, :], gw_ref[now]) * scale).astype(BF16)
            do_ref[now, rows, :] = do
            product = do.astype(F32) * o_ref[now, rows, :].astype(F32)
            high = product.astype(BF16)
            low = (product - high.astype(F32)).astype(BF16)
            delta_ref[now, :, rows] = dot_nt(pick, high) + dot_nt(pick, low)

        value = dot_nn(gbt_ref[...], o_ref[now]).astype(BF16)
        value = value.reshape(Z_DEV, Y_DEV, depth, width)

        hold_ref[now] = value

    serve(0)

    for ii in reversed(range(4)):
        @pl.when(i == ii)
        def _():
            first, last = ii * step, (ii + 1) * step
            do = do_ref[now, first:last, :]
            q = q_ref[now, first:last, :]
            v = v_ref[now, :last, :]
            lane = lax.broadcasted_iota(jnp.int32, (1, width), 1)
            dk, dv, dq = None, None, []
            for h in range(heads):
                low, high = h * HEAD_DIM, (h + 1) * HEAD_DIM
                here = (lane >= low) & (lane < high)
                p = p_ref[0, h, 0, :last, :]
                dp = dot_nt(v, jnp.where(here, do, jnp.zeros((), BF16)))
                ds = p * (dp - delta_ref[now, h : h + 1, first:last]).astype(BF16)
                part = dot_nn(p, do)
                dv = part if dv is None else jnp.where(lane < low, dv, part)
                part = dot_nn(ds, q)
                dk = part if dk is None else jnp.where(lane < low, dk, part)
                dq.append(dot_nn(kt_ref[now, low:high, :last], ds))
            if ii == 3:
                dkv_ref[now, 0] = dk
                dkv_ref[now, 1] = dv
            else:
                dkv_ref[now, 0, :last, :] += dk
                dkv_ref[now, 1, :last, :] += dv
            dk = dkv_ref[now, 0, first:last, :].astype(BF16)
            dv = dkv_ref[now, 1, first:last, :].astype(BF16)
            dq = (jnp.concatenate(dq, 0) * HEAD_DIM ** -0.5).astype(BF16).T
            dqkv_ref[now, first:last, :width] = dq
            dqkv_ref[now, first:last, width : 2 * width] = dk
            dqkv_ref[now, first:last, 2 * width :] = dv
            bqv_ref[mine, 0:1, :] += jnp.sum(dq.astype(F32), 0, keepdims=True)
            bqv_ref[mine, 1:2, :] += jnp.sum(dv.astype(F32), 0, keepdims=True)

            @pl.when(t >= 8)
            def _():
                da1_ref[first:last, :] += dot_nt(dqkv_ref[now, first:last, :], gq_ref[now])

    serve(1)

    @pl.when((t == 3) | (t == 7) | (t > 13))
    def _():
        @when(3)
        def _():
            fetch.wait()
            fetch_a1t.wait()

        @when(3)
        def _():
            da1_ref[...] = dot_nt(dqkv_ref[now], gq_ref[now])

        @when(7)
        def _():
            da1_ref[...] += dot_nt(dqkv_ref[now], gq_ref[now])

        value = dot_nn(a1t_ref[...], dqkv_ref[now]).reshape(Z_DEV, Y_DEV, depth, 3 * width)
        value = jnp.concatenate([value, hold_ref[now].astype(F32)], -1)
        for s in range(2):
            @when(3 + 11 * s)
            def _():
                if s:
                    core0[0].wait_send()
                stage0_ref[...] = value.astype(BF16)
                start(core0[s])

            @when(7 + 8 * s)
            def _():
                recv(core0[s])
                work0_ref[s] = (value + land0_ref[s].astype(F32)).astype(BF16)
                start(seg0.y[s])

    @pl.when((t > 8) & (t % 2 == 1))
    def _():
        rows = pl.ds(pl.multiple_of(i * step, step), step)
        xhat, r = norm_parts(own_ref[rows, :].astype(F32))
        da1 = da1_ref[rows, :]
        sums_ref[0, 0:1, :] += jnp.sum(da1 * xhat, 0, keepdims=True)
        sums_ref[0, 2:3, :] += jnp.sum(da1, 0, keepdims=True)
        dg = da1 * rows_ref[0:1, :]
        dv = r * (
            dg
            - jnp.mean(dg, -1, keepdims=True)
            - xhat * jnp.mean(dg * xhat, -1, keepdims=True)
        )
        own_ref[rows, :] = (dh1_ref[...] + dv).astype(BF16)
        for ii in range(4):
            @pl.when(i == ii)
            def _():
                out.send(ii)

    @when(15)
    def _():
        for s in range(4):
            sums_ref[0, 3:5, s * width : (s + 1) * width] = bqv_ref[s, 0:2, :]
        start(sum_core)
        out.pass_on(2)
        recv(sum_core)
        sums_ref[1] = sums_ref[0] + sumland_ref[0]
        start(sum_y)
        seg0.fold_y(1, 0)
        out.pass_on(1)
        seg0.fold_y(1, 1)
        recv(sum_y)
        sums_ref[2] = sums_ref[1] + sumland_ref[1]
        start(sum_z)
        seg0.fold_z(1)
        recv(sum_z)
        sums_ref[3] = (sums_ref[2] + sumland_ref[2]) + (sumland_ref[3] + sumland_ref[4])
        start(sum_x)
        part1_ref[...] = seg1.total()
        part2_ref[...] = seg2.total()
        seg0.send_x()
        layer.finish()
        out.pass_on(0)
        recv(sum_x)
        total_ref[...] = sums_ref[3] + sumland_ref[5]
        part0_ref[...] = seg0.total()
        out.finish()
        links.sent(core0[0])


def group_and_block(t):
    early = t < 8
    return (
        jnp.where(early, 1 - t // 4, 3 - t % 2),
        3 - jnp.where(early, t % 4, jnp.maximum(t - 8, 0) // 2),
    )


def run_fused_backward(
    tokens, gq, gw, rows, dh1, gb, gbt, q, v, kt, p, scale, o, a1t, layer, fold, work, early
):
    groups, n, _ = tokens.shape
    width = gw.shape[-1]
    heads = width // HEAD_DIM
    hidden = fold.shape[-1]
    depth = D // (Z_DEV * Y_DEV)
    step = n // 4

    p_spec = pl.BlockSpec(
        (1, heads, 1, n, step),
        lambda t: (group_and_block(t)[0], 0, group_and_block(t)[1], 0, 0),
    )

    copies = 2 * 12 + 2 + 15 + 2 * 11 + 6

    def landing(lanes, slots=1):
        return [
            pltpu.VMEM((slots, Z_DEV, depth, lanes), BF16),
            pltpu.VMEM((2, 3, depth, lanes), BF16), pltpu.VMEM((2, 2, depth, lanes), BF16),
            pltpu.VMEM((depth, lanes), BF16), pltpu.VMEM((depth, lanes), BF16),
        ]

    def working(lanes):
        block = (Z_DEV, Y_DEV, depth, lanes)
        return [pltpu.VMEM(block, BF16)] + [pltpu.VMEM((2,) + block, BF16)] * 2

    return pl.pallas_call(
        fused_backward,
        grid=(4 * groups,),
        in_specs=[
            ANY_WHOLE, ANY_WHOLE, ANY_WHOLE, VMEM_WHOLE,
            pl.BlockSpec((step, D), lambda t: (group_and_block(jnp.maximum(t, 8))[1], 0)),
            VMEM_WHOLE, ANY_WHOLE, ANY_WHOLE, ANY_WHOLE, ANY_WHOLE, p_spec,
            ANY_WHOLE, ANY_WHOLE, ANY_WHOLE, ANY_WHOLE, ANY_WHOLE, ANY_WHOLE, VMEM_WHOLE,
        ],
        out_specs=[ANY_WHOLE] * 2 + [VMEM_WHOLE] * 4,
        out_shape=[
            shaped(BF16, groups, n, D), shaped(BF16, groups, n, D),
            shaped(F32, depth, 4 * width), shaped(F32, depth, hidden),
            shaped(F32, depth, hidden), shaped(F32, 16, D),
        ],
        scratch_shapes=[
            pltpu.VMEM((2, D, 3 * width), BF16), pltpu.VMEM((2, D, width), BF16),
            pltpu.VMEM((2, n, width), BF16), pltpu.VMEM((2, n, width), BF16),
            pltpu.VMEM((2, width, n), BF16), pltpu.VMEM((2, 8, n), F32),
            pltpu.VMEM((2, n, width), BF16),
            pltpu.VMEM((D, n), BF16), pltpu.VMEM((D, n), BF16), pltpu.VMEM((n, D), BF16),
            pltpu.VMEM((2, Z_DEV, depth, hidden), BF16),
            pltpu.VMEM((2, Z_DEV, Y_DEV, depth, hidden), BF16),
            pltpu.VMEM((2, n, width), BF16),
            pltpu.VMEM((2, 8, n), F32), pltpu.VMEM((2, 2, n, width), F32),
            pltpu.VMEM((2, n, 3 * width), BF16),
            pltpu.VMEM((2, Z_DEV, Y_DEV, depth, width), BF16), pltpu.VMEM((n, D), F32),
            pltpu.VMEM((n, D), BF16), pltpu.VMEM((n, D), BF16), pltpu.VMEM((n, D), BF16),
            pltpu.VMEM((groups, 8, width), F32),
        ]
        + [pltpu.VMEM((2, Z_DEV, depth, hidden), BF16)] + landing(hidden) + landing(hidden)
        + working(4 * width) + landing(4 * width, 2)
        + [
            pltpu.VMEM((4, 16, D), F32), pltpu.VMEM((6, 16, D), F32),
            pltpu.SemaphoreType.DMA((copies,)), pltpu.SemaphoreType.DMA((copies,)),
            pltpu.SemaphoreType.DMA((6,)), pltpu.SemaphoreType.DMA((2, 2, 4)),
            pltpu.SemaphoreType.DMA((2, 7)),
        ],
        compiler_params=pltpu.CompilerParams(
            vmem_limit_bytes=VMEM_LIMIT, collective_id=2, has_side_effects=True
        ),
        name="fused_backward",
    )(tokens, gq, gw, rows, dh1, gb, gbt, q, v, kt, p, scale, o, a1t, layer, fold, work, early)


def place_gradients(
    tie_ref, sums_ref, part0_ref, part1_ref, part2_ref, near_out_ref,
    near_grad_ref, far_out_ref, far_grad_ref, gains_ref, bias_ref, in_ref, out_ref, expand_ref,
    project_ref, chosen_ref,
):
    t = pl.program_id(0)
    far_out_ref[...] = near_out_ref[...]
    far_grad_ref[...] = near_grad_ref[...]
    own = gains_ref.shape[-1]
    width = part0_ref.shape[-1] // 4
    kinds = [tie_ref[0], tie_ref[1], tie_ref[2], tie_ref[3]]

    @pl.when(t == 0)
    def _():
        first = (lax.axis_index("dp") * 4 + lax.axis_index("tensor")) * own
        feature = lax.broadcasted_iota(jnp.int32, (D, 128), 0)
        lane = lax.broadcasted_iota(jnp.int32, (D, 128), 1)
        chosen = ((feature == first + lane) & (lane < own)).astype(F32)
        chosen_ref[...] = lax.dot_general(
            sums_ref[...], chosen, (((1,), (0,)), ((), ())),
            precision=lax.Precision.HIGHEST, preferred_element_type=F32,
        )
        row = lax.broadcasted_iota(jnp.int32, (NSRC, own), 0)
        for i, kind in enumerate([0, 0, 0, 1, 2, 3, 2, 2, 2, 2]):
            value = chosen_ref[2 + i : 3 + i, :own]
            bias_ref[i] = jnp.where(row == kinds[kind], value, 0.0)

    @pl.when(t < NSRC)
    def _():
        def here(kind, value):
            return jnp.where(kinds[kind] == t, value, jnp.zeros_like(value))

        gains_ref[0, 0:1] = here(0, chosen_ref[0:1, :own])
        gains_ref[0, 1:2] = here(2, chosen_ref[1:2, :own])
        for j in range(3):
            in_ref[0, j] = here(0, part0_ref[:, j * width : (j + 1) * width])
        out_ref[0] = here(1, part0_ref[:, 3 * width :].T)
        expand_ref[0] = here(2, part1_ref[...])
        project_ref[0] = here(3, part2_ref[...])


def run_place_gradients(tie, sums, part0, part1, part2, out, grad, like):
    slots, n, _ = grad.shape
    gains, biases, w_in, w_out, w_expand, w_project = [item.shape for item in like]
    shapes = [
        gains, (biases[1], biases[0], biases[2]), w_in, w_out, w_expand,
        (w_project[0], w_project[2], w_project[1]),
    ]

    def source(shape):
        return pl.BlockSpec(
            (1,) + shape[1:], lambda t: (jnp.minimum(t, NSRC - 1),) + (0,) * (len(shape) - 1)
        )

    out, grad, gains, biases, w_in, w_out, w_expand, w_project = pl.pallas_call(
        place_gradients,
        grid=(slots,),
        in_specs=[SMEM_WHOLE] + [VMEM_WHOLE] * 4 + [group(n, D), group(n, D)],
        out_specs=[group(n, D), group(n, D), source(shapes[0]), VMEM_WHOLE]
        + [source(shape) for shape in shapes[2:]],
        out_shape=[shaped(BF16, slots, n, D)] * 2 + [shaped(F32, *item) for item in shapes],
        scratch_shapes=[pltpu.VMEM((16, 128), F32)],
        compiler_params=pltpu.CompilerParams(vmem_limit_bytes=VMEM_LIMIT),
        name="place_gradients",
    )(tie, sums, part0, part1, part2, out, grad)
    biases = biases.transpose(1, 0, 2)
    return out, grad, gains, biases, w_in, w_out, w_expand, w_project.transpose(0, 2, 1)


def plain_step(
    tokens, lengths, tie_map, norm_gains, bias_rows, attention_in, attention_out,
    expand_weight, project_weight, cotangent,
):
    slot_rows = tokens.shape[0] // lengths.shape[0]
    me = lax.axis_index("tensor")
    in_local = lax.dynamic_index_in_dim(attention_in, tie_map[0], 0, keepdims=False)
    out_local = lax.dynamic_index_in_dim(attention_out, tie_map[1], 0, keepdims=False)
    expand_local = lax.dynamic_index_in_dim(expand_weight, tie_map[2], 0, keepdims=False)
    project_local = lax.dynamic_index_in_dim(project_weight, tie_map[3], 0, keepdims=False)
    local0 = jnp.concatenate([in_local, out_local.T[None]], 0)
    row_kinds = jnp.array([0, 0, 0, 1, 2, 3] + [2] * (FF // D), dtype=jnp.int32)
    gain_kinds = jnp.array([0, 2], dtype=jnp.int32)
    gain_pick = norm_gains[tie_map[gain_kinds], jnp.arange(2)]
    bias_pick = bias_rows[tie_map[row_kinds], jnp.arange(row_kinds.shape[0])]
    vectors = jnp.concatenate([gain_pick, bias_pick], 0)
    x = lax.dynamic_slice_in_dim(tokens, me * slot_rows, slot_rows, 0)
    cot = lax.dynamic_slice_in_dim(cotangent, me * slot_rows, slot_rows, 0)
    length = lax.dynamic_slice_in_dim(lengths, me, 1, 0)
    rows = lax.all_gather(vectors, ("dp", "tensor"), axis=1, tiled=True).astype(F32)
    rows = jnp.concatenate([rows, jnp.zeros((4, D), F32)], 0)

    def gathered(piece, axis):
        piece = lax.all_gather(piece, "dp", axis=axis, tiled=True)
        return lax.all_gather(piece, "tensor", axis=0)

    g0 = gathered(local0, 1)
    g1 = gathered(expand_local, 0)
    g2 = gathered(project_local.T, 0)
    groups, width = g0.shape[0], g0.shape[-1]
    bqv = rows[3:5].reshape(2, groups, width).transpose(1, 0, 2)
    q, v, kt, p, o, a1t, h1, a2, a2t = run_attention_forward(length, x, g0, rows, bqv)
    out, d1, d2, dh1, gb, gbt, sums = run_feed_forward(length, cot, a2, a2t, h1, g1, g2, rows)
    d0, xg, sums_in, sums_qv = run_attention_backward(
        x, g0, rows, dh1, gb, gbt, q, v, kt, p, o, a1t
    )
    layer_out = lax.all_gather(out, "tensor", axis=0, tiled=True)
    tokens_grad = lax.all_gather(xg, "tensor", axis=0, tiled=True)

    def scattered(piece, axis):
        piece = lax.psum_scatter(piece, "tensor", scatter_dimension=0)
        return lax.psum_scatter(piece, "dp", scatter_dimension=axis, tiled=True).astype(F32)

    part0 = scattered(d0, 1)
    part1 = scattered(d1, 0)
    part2 = scattered(d2, 0)
    qv = sums_qv[:, :2].transpose(1, 0, 2).reshape(2, D)
    sums = jnp.concatenate(
        [sums_in[0:1], sums[1:2], sums_in[1:2], qv, sums[5:12]], 0
    )
    sums = lax.psum_scatter(sums, ("dp", "tensor"), scatter_dimension=1, tiled=True)
    return layer_out, tokens_grad, *placed(tie_map, sums, part0, part1, part2)


def fused_step(
    tokens, lengths, tie_map, norm_gains, bias_rows, attention_in, attention_out,
    expand_weight, project_weight, cotangent,
):
    slots = lengths.shape[0]
    tokens = tokens.reshape(slots, -1, D)
    cotangent = cotangent.reshape(slots, -1, D)
    gq, gw, g1, g2, rows, q, v, kt, p, scale, o, a1t, h1, a2, a2t = run_fused_forward(
        tie_map, lengths, tokens, norm_gains, bias_rows, attention_in, attention_out,
        expand_weight, project_weight,
    )
    layer, fold, work, dh1, gb, gbt, early = run_fused_feed_forward(
        lengths, cotangent, a2, a2t, h1, g1, g2, rows
    )
    grad, out, part0, part1, part2, sums = run_fused_backward(
        tokens, gq, gw, rows, dh1, gb, gbt, q, v, kt, p, scale, o, a1t, layer, fold,
        work, early,
    )
    out, grad, *placed_grads = run_place_gradients(
        tie_map, sums, part0, part1, part2, out, grad,
        (norm_gains, bias_rows, attention_in, attention_out, expand_weight, project_weight),
    )
    return out.reshape(-1, D), grad.reshape(-1, D), *placed_grads


def placed(tie_map, sums, part0, part1, part2):
    source = jnp.arange(NSRC, dtype=jnp.int32)

    def place(piece, which):
        pick = (source == tie_map[which]).reshape((NSRC,) + (1,) * piece.ndim)
        return jnp.where(pick, piece[None], 0.0)

    def place_rows(piece, kinds):
        pick = source[:, None] == tie_map[jnp.array(kinds, dtype=jnp.int32)][None, :]
        return jnp.where(pick[:, :, None], piece[None], 0.0)

    return (
        place_rows(sums[:2], [0, 2]),
        place_rows(sums[2:], [0, 0, 0, 1, 2, 3] + [2] * (FF // D)),
        place(part0[:3], 0),
        place(part0[3].T, 1),
        place(part1, 2),
        place(part2.T, 3),
    )


def solution(mesh):
    fused = mesh.shape["dp"] == Z_DEV * Y_DEV and mesh.shape["tensor"] == X_DEV * C_DEV
    return jax.shard_map(
        fused_step if fused else plain_step,
        mesh=mesh,
        in_specs=(
            P("dp", None),
            P("dp"),
            P(),
            P(None, None, ("dp", "tensor")),
            P(None, None, ("dp", "tensor")),
            P(None, None, "dp", "tensor"),
            P(None, "tensor", "dp"),
            P(None, "dp", "tensor"),
            P(None, "tensor", "dp"),
            P("dp", None),
        ),
        out_specs=(
            P("dp", None),
            P("dp", None),
            P(None, None, ("dp", "tensor")),
            P(None, None, ("dp", "tensor")),
            P(None, None, "dp", "tensor"),
            P(None, "tensor", "dp"),
            P(None, "dp", "tensor"),
            P(None, "tensor", "dp"),
        ),
        check_vma=False,
    )
```

```python
import jax
import jax.numpy as jnp
from jax import lax
from jax.experimental import pallas as pl
from jax.experimental.pallas import tpu as pltpu
from jax.sharding import PartitionSpec as P

D = 768
HEAD_DIM = 64
FF = 3072
NSRC = 4
EPS = 1e-05
MASKED = -1e30
F32 = jnp.float32
BF16 = jnp.bfloat16
VMEM_LIMIT = 60 * 1024 * 1024


def dot_nn(a, b):
    return lax.dot_general(a, b, (((1,), (0,)), ((), ())), preferred_element_type=F32)


def dot_nt(a, b):
    return lax.dot_general(a, b, (((1,), (1,)), ((), ())), preferred_element_type=F32)


def norm_parts(v):
    center = jnp.mean(v, -1, keepdims=True)
    centered = v - center
    r = lax.rsqrt(jnp.mean(centered * centered, -1, keepdims=True) + EPS)
    return centered * r, r


def head_mask(shape, h):
    lane = lax.broadcasted_iota(jnp.int32, shape, 1)
    return (lane >= h * HEAD_DIM) & (lane < (h + 1) * HEAD_DIM)


def blocks(total, size):
    return [slice(i * size, (i + 1) * size) for i in range(total // size)]


def attention_forward(
    len_ref, x_ref, g_ref, rows_ref, bqv_ref,
    q_ref, v_ref, kt_ref, p_ref, o_ref, a1t_ref, h1_ref, a2_ref, a2t_ref,
    a1_ref, k_ref, vt_ref, ot_ref, attn_ref,
):
    t = pl.program_id(0)
    n = x_ref.shape[0]
    width = g_ref.shape[-1]
    heads = width // HEAD_DIM
    step = 256
    length = len_ref[0]

    @pl.when(t == 0)
    def _():
        @pl.loop(0, n // step)
        def _(b):
            rows = pl.ds(pl.multiple_of(b * step, step), step)
            xhat, _ = norm_parts(x_ref[rows, :].astype(F32))
            a1 = xhat * rows_ref[0:1, :] + rows_ref[2:3, :]
            a1_ref[rows, :] = a1.astype(BF16)
            a1t_ref[:, rows] = a1.astype(BF16).T
            attn_ref[rows, :] = x_ref[rows, :].astype(F32) + rows_ref[5:6, :]

    @pl.loop(0, n // step)
    def _(b):
        rows = pl.ds(pl.multiple_of(b * step, step), step)
        a1 = a1_ref[rows, :]
        q = (dot_nn(a1, g_ref[0, 0]) + bqv_ref[0, 0:1, :]).astype(BF16)
        q_ref[0, rows, :] = q * jnp.asarray(HEAD_DIM ** -0.5, BF16)
        k = dot_nn(a1, g_ref[0, 1]).astype(BF16)
        k_ref[rows, :] = k
        kt_ref[0, :, rows] = k.T
        v = (dot_nn(a1, g_ref[0, 2]) + bqv_ref[0, 1:2, :]).astype(BF16)
        v_ref[0, rows, :] = v
        vt_ref[:, rows] = v.T

    for h in range(heads):
        k = k_ref[...]
        k = jnp.where(head_mask(k.shape, h), k, jnp.zeros_like(k))
        for b in range(n // step):
            first, last = b * step, (b + 1) * step
            q = q_ref[0, first:last, :]
            key = lax.broadcasted_iota(jnp.int32, (last, step), 0)
            query = lax.broadcasted_iota(jnp.int32, (step, step), 1) + first
            s = dot_nt(k[:last], q)
            near = jnp.where(
                (key[first:] <= query) & (key[first:] < length), s[first:], MASKED
            )
            if b:
                far = jnp.where(key[:first] < length, s[:first], MASKED)
                top = jnp.maximum(
                    jnp.max(far, 0, keepdims=True), jnp.max(near, 0, keepdims=True)
                )
                e_far = jnp.exp(far - top)
                e_near = jnp.exp(near - top)
                total = jnp.sum(e_far, 0, keepdims=True) + jnp.sum(e_near, 0, keepdims=True)
                scale = 1.0 / total
                p_ref[0, h, :first, first:last] = (e_far * scale).astype(BF16)
            else:
                top = jnp.max(near, 0, keepdims=True)
                e_near = jnp.exp(near - top)
                scale = 1.0 / jnp.sum(e_near, 0, keepdims=True)
            p_ref[0, h, first:last, first:last] = (e_near * scale).astype(BF16)
            ot_ref[h * HEAD_DIM : (h + 1) * HEAD_DIM, first:last] = dot_nn(
                vt_ref[h * HEAD_DIM : (h + 1) * HEAD_DIM, :last],
                p_ref[0, h, :last, first:last],
            ).astype(BF16)

    @pl.loop(0, n // step)
    def _(b):
        rows = pl.ds(pl.multiple_of(b * step, step), step)
        o = ot_ref[:, rows].T
        o_ref[0, rows, :] = o
        attn_ref[rows, :] += dot_nt(o, g_ref[0, 3])

    @pl.when(t == pl.num_programs(0) - 1)
    def _():
        @pl.loop(0, n // step)
        def _(b):
            rows = pl.ds(pl.multiple_of(b * step, step), step)
            h1 = attn_ref[rows, :]
            h1_ref[rows, :] = h1
            xhat, _ = norm_parts(h1)
            a2 = (xhat * rows_ref[1:2, :] + rows_ref[6:7, :]).astype(BF16)
            a2_ref[rows, :] = a2
            a2t_ref[:, rows] = a2.T


SQRT_2_PI = 0.7978845608028654


def feed_forward_both(
    len_ref, c_ref, a2_ref, a2t_ref, h1_ref, w1_ref, w2_ref, rows_ref,
    out_ref, d1_ref, d2_ref, dh1_ref, gb_ref, gbt_ref, sums_ref,
    gf_ref, gft_ref, feed_ref, da2_ref, h_ref, df_ref,
):
    t = pl.program_id(0)
    n = c_ref.shape[0]
    step = 256
    length = len_ref[0]

    @pl.when(t == 0)
    def _():
        sums_ref[...] = jnp.zeros_like(sums_ref)

        @pl.loop(0, n // step)
        def _(b):
            rows = pl.ds(pl.multiple_of(b * step, step), step)
            place = b * step + lax.broadcasted_iota(jnp.int32, (step, 1), 0)
            live = (place < length).astype(F32)
            g = (c_ref[rows, :].astype(F32) * live).astype(BF16)
            gf_ref[rows, :] = g
            gft_ref[:, rows] = g.T
            sums_ref[7:8, :] += jnp.sum(g.astype(F32), 0, keepdims=True)

    bias = rows_ref[pl.ds(8 + t, 1), :]

    @pl.loop(0, n // step)
    def _(b):
        rows = pl.ds(pl.multiple_of(b * step, step), step)
        f = dot_nn(a2_ref[rows, :], w1_ref[0]) + bias
        dh = dot_nn(gf_ref[rows, :], w2_ref[0])
        f2 = f * f
        th = jnp.tanh(f * (SQRT_2_PI + (SQRT_2_PI * 0.044715) * f2))
        half = 0.5 + 0.5 * th
        h = (f * half).astype(BF16)
        slope = half + f * (0.5 - 0.5 * th * th) * (
            SQRT_2_PI + (3 * SQRT_2_PI * 0.044715) * f2
        )
        df = (dh * slope).astype(BF16)
        h_ref[rows, :] = h
        df_ref[rows, :] = df
        sums_ref[pl.ds(8 + t, 1), :] += jnp.sum(df.astype(F32), 0, keepdims=True)
        feed = dot_nt(h, w2_ref[0])
        da2 = dot_nt(df, w1_ref[0])

        @pl.when(t == 0)
        def _():
            feed_ref[rows, :] = feed
            da2_ref[rows, :] = da2

        @pl.when(t > 0)
        def _():
            feed_ref[rows, :] += feed
            da2_ref[rows, :] += da2

    @pl.loop(0, D // step)
    def _(b):
        rows = pl.ds(pl.multiple_of(b * step, step), step)
        d1_ref[0, rows, :] = dot_nn(a2t_ref[rows, :], df_ref[...]).astype(BF16)
        d2_ref[0, rows, :] = dot_nn(gft_ref[rows, :], h_ref[...]).astype(BF16)

    @pl.when(t == pl.num_programs(0) - 1)
    def _():
        @pl.loop(0, n // step)
        def _(b):
            rows = pl.ds(pl.multiple_of(b * step, step), step)
            place = b * step + lax.broadcasted_iota(jnp.int32, (step, 1), 0)
            live = (place < length).astype(F32)
            h1 = h1_ref[rows, :]
            out_ref[rows, :] = (live * (h1 + (feed_ref[rows, :] + rows_ref[7:8, :]))).astype(BF16)
            xhat, r = norm_parts(h1)
            da2 = da2_ref[rows, :]
            sums_ref[1:2, :] += jnp.sum(da2 * xhat, 0, keepdims=True)
            sums_ref[6:7, :] += jnp.sum(da2, 0, keepdims=True)
            dg = da2 * rows_ref[1:2, :]
            dv = r * (
                dg
                - jnp.mean(dg, -1, keepdims=True)
                - xhat * jnp.mean(dg * xhat, -1, keepdims=True)
            )
            dh1 = live * c_ref[rows, :].astype(F32) + dv
            dh1_ref[rows, :] = dh1
            gb = dh1.astype(BF16)
            gb_ref[rows, :] = gb
            gbt_ref[:, rows] = gb.T
            sums_ref[5:6, :] += jnp.sum(gb.astype(F32), 0, keepdims=True)


def attention_backward(
    x_ref, g_ref, rows_ref, dh1_ref, gb_ref, gbt_ref, q_ref, v_ref, kt_ref, p_ref,
    o_ref, a1t_ref,
    d0_ref, xg_ref, sums_ref, bqv_ref,
    do_ref, delta_ref, dqt_ref, dq_ref, dk_ref, dv_ref, da1_ref,
):
    t = pl.program_id(0)
    n = x_ref.shape[0]
    width = g_ref.shape[-1]
    heads = width // HEAD_DIM
    step = 256
    pick = (
        lax.broadcasted_iota(jnp.int32, (16, width), 1) // HEAD_DIM
        == lax.broadcasted_iota(jnp.int32, (16, width), 0)
    ).astype(BF16)

    @pl.loop(0, n // step)
    def _(b):
        rows = pl.ds(pl.multiple_of(b * step, step), step)
        do = dot_nn(gb_ref[rows, :], g_ref[0, 3]).astype(BF16)
        do_ref[rows, :] = do
        prod = do.astype(F32) * o_ref[0, rows, :].astype(F32)
        high = prod.astype(BF16)
        low = (prod - high.astype(F32)).astype(BF16)
        delta_ref[:, rows] = dot_nt(pick, high) + dot_nt(pick, low)

    dqt_ref[...] = jnp.zeros_like(dqt_ref)
    for b in range(n // step):
        first, last = b * step, (b + 1) * step
        do = do_ref[first:, :]
        q = q_ref[0, first:, :]
        v = v_ref[0, first:last, :]
        dk, dv = None, None
        for h in range(heads):
            mine = head_mask((1, width), h)
            zero = jnp.zeros((), BF16)
            p = p_ref[0, h, first:last, first:]
            dp = dot_nt(jnp.where(mine, v, zero), do)
            ds = (p.astype(F32) * (dp - delta_ref[h : h + 1, first:])).astype(BF16)
            part = dot_nn(p, jnp.where(mine, do, zero))
            dv = part if dv is None else dv + part
            part = dot_nn(ds, jnp.where(mine, q, zero))
            dk = part if dk is None else dk + part
            head = slice(h * HEAD_DIM, (h + 1) * HEAD_DIM)
            dqt_ref[head, first:] += dot_nn(kt_ref[0, head, first:last], ds)
        dk_ref[first:last, :] = dk.astype(BF16)
        dv_ref[first:last, :] = dv.astype(BF16)

    @pl.when(t == 0)
    def _():
        da1_ref[...] = jnp.zeros_like(da1_ref)

    bqv_ref[...] = jnp.zeros_like(bqv_ref)

    @pl.loop(0, n // step)
    def _(b):
        rows = pl.ds(pl.multiple_of(b * step, step), step)
        dq = (dqt_ref[:, rows] * HEAD_DIM ** -0.5).astype(BF16).T
        dk = dk_ref[rows, :]
        dv = dv_ref[rows, :]
        dq_ref[rows, :] = dq
        bqv_ref[0, 0:1, :] += jnp.sum(dq.astype(F32), 0, keepdims=True)
        bqv_ref[0, 1:2, :] += jnp.sum(dv.astype(F32), 0, keepdims=True)
        da1_ref[rows, :] += (
            dot_nt(dq, g_ref[0, 0]) + dot_nt(dk, g_ref[0, 1]) + dot_nt(dv, g_ref[0, 2])
        )

    @pl.loop(0, D // step)
    def _(b):
        rows = pl.ds(pl.multiple_of(b * step, step), step)
        a1t = a1t_ref[rows, :]
        d0_ref[0, 0, rows, :] = dot_nn(a1t, dq_ref[...]).astype(BF16)
        d0_ref[0, 1, rows, :] = dot_nn(a1t, dk_ref[...]).astype(BF16)
        d0_ref[0, 2, rows, :] = dot_nn(a1t, dv_ref[...]).astype(BF16)
        d0_ref[0, 3, rows, :] = dot_nn(gbt_ref[rows, :], o_ref[0]).astype(BF16)

    @pl.when(t == pl.num_programs(0) - 1)
    def _():
        sums_ref[...] = jnp.zeros_like(sums_ref)

        @pl.loop(0, n // step)
        def _(b):
            rows = pl.ds(pl.multiple_of(b * step, step), step)
            xhat, r = norm_parts(x_ref[rows, :].astype(F32))
            da1 = da1_ref[rows, :]
            sums_ref[0:1, :] += jnp.sum(da1 * xhat, 0, keepdims=True)
            sums_ref[1:2, :] += jnp.sum(da1, 0, keepdims=True)
            dg = da1 * rows_ref[0:1, :]
            dv = r * (
                dg
                - jnp.mean(dg, -1, keepdims=True)
                - xhat * jnp.mean(dg * xhat, -1, keepdims=True)
            )
            xg_ref[rows, :] = (dh1_ref[rows, :] + dv).astype(BF16)


def whole(*shape):
    return pl.BlockSpec(shape, lambda t: (0,) * len(shape))


def group(*shape):
    return pl.BlockSpec((1,) + shape, lambda t: (t,) + (0,) * len(shape))


def shaped(dtype, *shape):
    return jax.ShapeDtypeStruct(shape, dtype)


SMEM_WHOLE = pl.BlockSpec(memory_space=pltpu.SMEM)


def run_attention_forward(length, x, g0, rows, bqv):
    n = x.shape[0]
    groups, _, _, width = g0.shape
    heads = width // HEAD_DIM
    return pl.pallas_call(
        attention_forward,
        grid=(groups,),
        in_specs=[SMEM_WHOLE, whole(n, D), group(4, D, width), whole(16, D), group(2, width)],
        out_specs=[
            group(n, width), group(n, width), group(width, n), group(heads, n, n),
            group(n, width), whole(D, n), whole(n, D), whole(n, D), whole(D, n),
        ],
        out_shape=[
            shaped(BF16, groups, n, width), shaped(BF16, groups, n, width),
            shaped(BF16, groups, width, n), shaped(BF16, groups, heads, n, n),
            shaped(BF16, groups, n, width), shaped(BF16, D, n), shaped(F32, n, D),
            shaped(BF16, n, D), shaped(BF16, D, n),
        ],
        scratch_shapes=[
            pltpu.VMEM((n, D), BF16), pltpu.VMEM((n, width), BF16),
            pltpu.VMEM((width, n), BF16), pltpu.VMEM((width, n), BF16),
            pltpu.VMEM((n, D), F32),
        ],
        compiler_params=pltpu.CompilerParams(vmem_limit_bytes=VMEM_LIMIT),
        name="attention_forward",
    )(length, x, g0, rows, bqv)


def run_feed_forward(length, cot, a2, a2t, h1, g1, g2, rows):
    n = cot.shape[0]
    groups, _, width = g1.shape
    return pl.pallas_call(
        feed_forward_both,
        grid=(groups,),
        in_specs=[
            SMEM_WHOLE, whole(n, D), whole(n, D), whole(D, n), whole(n, D),
            group(D, width), group(D, width), whole(16, D),
        ],
        out_specs=[
            whole(n, D), group(D, width), group(D, width), whole(n, D), whole(n, D),
            whole(D, n), whole(16, D),
        ],
        out_shape=[
            shaped(BF16, n, D), shaped(BF16, groups, D, width), shaped(BF16, groups, D, width),
            shaped(F32, n, D), shaped(BF16, n, D), shaped(BF16, D, n), shaped(F32, 16, D),
        ],
        scratch_shapes=[
            pltpu.VMEM((n, D), BF16), pltpu.VMEM((D, n), BF16), pltpu.VMEM((n, D), F32),
            pltpu.VMEM((n, D), F32), pltpu.VMEM((n, width), BF16), pltpu.VMEM((n, width), BF16),
        ],
        compiler_params=pltpu.CompilerParams(vmem_limit_bytes=VMEM_LIMIT),
        name="feed_forward_both",
    )(length, cot, a2, a2t, h1, g1, g2, rows)


def run_attention_backward(x, g0, rows, dh1, gb, gbt, q, v, kt, p, o, a1t):
    n = x.shape[0]
    groups, _, _, width = g0.shape
    heads = width // HEAD_DIM
    return pl.pallas_call(
        attention_backward,
        grid=(groups,),
        in_specs=[
            whole(n, D), group(4, D, width), whole(16, D), whole(n, D), whole(n, D),
            whole(D, n), group(n, width), group(n, width), group(width, n),
            group(heads, n, n), group(n, width), whole(D, n),
        ],
        out_specs=[group(4, D, width), whole(n, D), whole(8, D), group(8, width)],
        out_shape=[
            shaped(BF16, groups, 4, D, width), shaped(BF16, n, D), shaped(F32, 8, D),
            shaped(F32, groups, 8, width),
        ],
        scratch_shapes=[
            pltpu.VMEM((n, width), BF16), pltpu.VMEM((16, n), F32), pltpu.VMEM((width, n), F32),
            pltpu.VMEM((n, width), BF16), pltpu.VMEM((n, width), BF16),
            pltpu.VMEM((n, width), BF16), pltpu.VMEM((n, D), F32),
        ],
        compiler_params=pltpu.CompilerParams(vmem_limit_bytes=VMEM_LIMIT),
        name="attention_backward",
    )(x, g0, rows, dh1, gb, gbt, q, v, kt, p, o, a1t)


Z_DEV, Y_DEV, X_DEV, C_DEV = 4, 2, 2, 2


class Place:
    def __init__(self):
        dp, self.t = lax.axis_index("dp"), lax.axis_index("tensor")
        self.dp = dp
        self.z, self.y = dp // 2, dp % 2
        self.x, self.c = self.t // 2, self.t % 2
        self.other_y = 1 - self.y
        self.zs = [
            self.z,
            self.z + 1 - 2 * (self.z % 2),
            self.z + 2 - 4 * (self.z // 2),
            3 - self.z,
        ]
        self.ts = [
            self.t,
            self.t + 1 - 2 * (self.t % 2),
            self.t + 2 - 4 * (self.t // 2),
            3 - self.t,
        ]
        self.to_z = [dict(dp=z * 2 + self.y) for z in self.zs]
        self.to_y = dict(dp=self.z * 2 + self.other_y)
        self.to_x = dict(tensor=self.ts[2])
        self.same_t = self.to_z[1:] + [dict(dp=z * 2 + self.other_y) for z in self.zs]
        self.same_dp = [dict(tensor=t) for t in self.ts[1:]]
        self.to_core = dict(tensor=self.ts[1])

    def group(self, k):
        return lax.select(
            k == 0, self.ts[0],
            lax.select(k == 1, self.ts[1], lax.select(k == 2, self.ts[2], self.ts[3])),
        )

    def greet(self, others=None):
        barrier = pltpu.get_barrier_semaphore()
        others = others or self.to_z[1:] + [self.to_y, self.to_x, self.to_core]
        for device in others:
            pl.semaphore_signal(
                barrier, inc=1, device_id=device, device_id_type=pl.DeviceIdType.MESH
            )
        pl.semaphore_wait(barrier, len(others))


class Pieces:
    def __init__(self, whole, pieces):
        self.whole, self.pieces = whole, pieces

    def start(self):
        for piece in self.pieces:
            piece.start()

    def wait_recv(self):
        self.whole.wait_recv()

    def wait_send(self):
        self.whole.wait_send()


class Links:
    def __init__(self, send_sem, recv_sem):
        self.send_sem, self.recv_sem = send_sem, recv_sem
        self.copies = []

    def add(self, device, src, dst, parts=1, axis=0):
        number = len(self.copies)

        def make(src, dst):
            return pltpu.make_async_remote_copy(
                src_ref=src,
                dst_ref=dst,
                send_sem=self.send_sem.at[number],
                recv_sem=self.recv_sem.at[number],
                device_id=device,
                device_id_type=pl.DeviceIdType.MESH,
            )

        size = src.shape[axis] // parts
        cuts = [(slice(None),) * axis + (pl.ds(i * size, size),) for i in range(parts)]
        copy = Pieces(make(src, dst), [make(src.at[cut], dst.at[cut]) for cut in cuts])
        self.copies.append(copy)
        return copy

    def sent(self, *apart):
        for copy in self.copies:
            if all(copy is not other for other in apart):
                copy.wait_send()


def flat(copies):
    for item in copies:
        if isinstance(item, list):
            yield from flat(item)
        else:
            yield item


def start(*copies):
    for copy in flat(copies):
        copy.start()


def recv(*copies):
    for copy in flat(copies):
        copy.wait_recv()


class Gather:
    def __init__(self, links, place, own, full, order, single=True, last=True):
        every = slice(None)
        y, other = place.y, place.other_y

        def same(device, k, yy, to):
            return links.add(device, full(k, every, yy), full(to, every, yy), Z_DEV)

        def along_z(k, yy, block):
            here, passed = full(k, place.z, yy), full(k, place.zs[2], yy)
            return [
                links.add(place.to_z[1], block, here),
                links.add(place.to_z[2], block, here),
                links.add(place.to_z[1], passed, passed),
            ]

        if order != WHOLE:
            self.z = along_z(0, y, own)
        if order == X_Z_Y:
            self.first = [links.add(place.to_x, own, full(2, place.z, y), 2)]
            self.far = along_z(2, y, full(2, place.z, y))
            blocks = [(0, y), (2, y), (0, other), (2, other)]
        else:
            blocks = [(0, y), (0, other), (2, y), (2, other)]
        if order == Y_Z_X:
            self.first = [links.add(place.to_y, own, full(0, place.z, y), 2)]
            self.far = along_z(0, other, full(0, place.z, other))
        if order == Z_Y_X and single:
            self.first = [same(place.to_y, 0, y, 0)]
        if order == Z_Y_X and not single:
            self.first = [links.add(place.to_y, own, full(0, place.z, y))]
            for k in range(1, 4):
                block = full(0, place.zs[k], y)
                self.first.append(links.add(place.to_y, block, block))
            return
        self.second = [
            same(place.to_y, k, yy, k) if order == X_Z_Y else same(place.to_x, k, yy, 2)
            for k, yy in blocks[: 2 if last else 1]
        ]
        if not last:
            blocks = [block for block in blocks if block[0] == 0]
        self.core = [same(place.to_core, k, yy, k + 1) for k, yy in blocks]


Z_Y_X, Y_Z_X, X_Z_Y, WHOLE = range(4)


def fused_forward(
    tie_ref, len_ref, tokens_ref, gains_ref, bias_ref, in_ref, out_ref, expand_ref,
    project_ref,
    gq_ref, gw_ref, flat1_ref, flat2_ref, rows_ref,
    q_ref, v_ref, kt_ref, p_ref, scale_ref, o_ref, a1t_out, h1_out, a2_out, a2t_out,
    own0_ref, own1_ref, own2_ref, square_ref, vec_ref,
    all0_ref, w1_ref, w2_ref, vecs_ref, bqv_ref, x_ref, a1_ref, k_ref, qa_ref, vt_ref, ot_ref, a1t_ref, h1_ref, a2_ref, a2t_ref,
    send_sem, recv_sem, local_sem, flush_sem, row_sem,
):
    t, h = pl.program_id(0), pl.program_id(1)
    n, _ = x_ref.shape
    width = q_ref.shape[-1]
    heads = width // HEAD_DIM
    step = 256
    place = Place()
    length = len_ref[place.t]
    links = Links(send_sem, recv_sem)
    z, y, x, c = place.z, place.y, place.x, place.c
    mine_there = vecs_ref.at[z, y, x, c]
    column = vecs_ref.at[:, :, x, c]
    vec_one = [links.add(device, vec_ref, mine_there) for device in place.same_t]
    vec_two = [links.add(device, column, column) for device in place.same_dp]
    half = own0_ref.shape[0] // 2
    halves = []
    for i in range(2):
        rows = pl.ds(i * half, half)
        halves.append(Gather(
            links, place, own0_ref.at[rows],
            lambda k, z, y, rows=rows: all0_ref.at[k, z, y, rows], Z_Y_X, single=False,
        ))
    seg0 = Gather(links, place, own0_ref, lambda k, z, y: all0_ref.at[k, z, y], WHOLE)
    seg1 = Gather(
        links, place, own1_ref, lambda k, z, y: w1_ref.at[k, z, y], Y_Z_X, last=False
    )
    seg2 = Gather(
        links, place, own2_ref, lambda k, z, y: w2_ref.at[k, z, y], X_Z_Y, last=False
    )
    flush = [
        [
            pltpu.make_async_copy(ref.at[k], flat.at[k], flush_sem.at[i, k])
            for k in range(3)
        ]
        for i, (ref, flat) in enumerate([(w1_ref, flat1_ref), (w2_ref, flat2_ref)])
    ]
    put_a1t = pltpu.make_async_copy(a1t_ref, a1t_out, local_sem.at[0])
    put_a2t = pltpu.make_async_copy(a2t_ref, a2t_out, local_sem.at[1])
    puts = []
    for i in range(n // step):
        rows = pl.ds(i * step, step)
        puts.append([
            pltpu.make_async_copy(h1_ref.at[rows], h1_out.at[rows], row_sem.at[0, i]),
            pltpu.make_async_copy(a2_ref.at[rows], a2_out.at[rows], row_sem.at[1, i]),
        ])
    fetch = pltpu.make_async_copy(tokens_ref.at[place.t], x_ref, local_sem.at[2])

    def relay_z(copies):
        recv(copies[1])
        start(copies[2])

    def pass_own(seg):
        recv(seg.z[0], seg.z[2])
        start(seg.second[0], seg.core[0])

    def pass_second(seg):
        recv(seg.second)
        if seg is seg2:
            start(seg.core[1])

    def pass_first(seg):
        recv(seg.first)
        start(seg.far[1], seg.far[0])

    def pass_far(seg):
        recv(seg.far[0], seg.far[2])
        start(seg.core[1:] if seg is seg1 else [])

    def pass_core(seg, i):
        recv(seg.second[i])
        start(seg.core[2 + i])

    plan = [
        (0, 0, lambda: (pass_first(seg1), relay_z(seg2.z), pass_first(seg2))),
        (0, 3, lambda: (relay_z(seg1.z), pass_core(seg0, 0))),
        (1, 0, lambda: recv(seg0.core[:2])),
        (1, 1, lambda: relay_z(seg1.far)),
        (1, 3, lambda: pass_core(seg0, 1)),
        (1, 4, lambda: pass_own(seg2)),
        (2, 1, lambda: relay_z(seg2.far)),
        (2, 3, lambda: pass_own(seg1)),
        (3, 0, lambda: (recv(seg0.core[2:]), pass_far(seg1), flush[0][0].start())),
        (3, 2, lambda: (pass_second(seg2), flush[1][0].start())),
        (3, 3, lambda: (pass_far(seg2), flush[1][2].start())),
    ]

    def serve(points):
        for step, where, act in plan:
            if where in points:
                now = (t == step) & (h == max(where - 2, 0))
                pl.when(now)(lambda act=act: (act(), None)[1])

    @pl.when((t == 0) & (h == 0))
    def _():
        s0, s1, s2, s3 = tie_ref[0], tie_ref[1], tie_ref[2], tie_ref[3]
        fetch.start()
        square_ref[...] = jnp.zeros_like(square_ref)
        gain = gains_ref.shape[-1]
        square_ref[0:1, :gain] = gains_ref[s0].astype(F32)[0:1]
        square_ref[1:2, :gain] = gains_ref[s2].astype(F32)[1:2]
        kinds = [s0, s0, s0, s1, s2, s3, s2, s2, s2, s2]
        for i, source in enumerate(kinds):
            wide = bias_ref[i].astype(F32)
            here = lax.broadcasted_iota(jnp.int32, wide.shape, 0) == source
            square_ref[2 + i : 3 + i, :gain] = jnp.sum(
                jnp.where(here, wide, 0.0), 0, keepdims=True
            )
        vec_ref[...] = square_ref[...].T[:gain]
        for j in range(3):
            own0_ref[:, j * width : (j + 1) * width] = in_ref[s0, j]
        own0_ref[:, 3 * width :] = out_ref[s1].T
        place.greet(place.same_t + place.same_dp)
        start(vec_one)
        for part in halves:
            start(part.z[1], part.z[0], part.first[0])
        vecs_ref[z, y, x, c] = vec_ref[...]
        ones = lax.broadcasted_iota(jnp.int32, (vt_ref.shape[1] - HEAD_DIM, n), 0) == 0
        for h in range(heads):
            vt_ref[h, HEAD_DIM:, :] = ones.astype(BF16)
        all0_ref[0, z, y] = own0_ref[...]
        own1_ref[...] = expand_ref[s2]
        own2_ref[...] = project_ref[s3]
        w1_ref[0, z, y] = own1_ref[...]
        w2_ref[0, z, y] = own2_ref[...]
        recv(vec_one)
        start(vec_two)
        for part in halves:
            relay_z(part.z)
            start(part.first[2])
        for part in halves:
            recv(part.z[0])
            start(part.first[1])
        start(seg2.z[1])
        recv(vec_two)
        start(seg2.first)
        vecs = vecs_ref[...].reshape(D, vecs_ref.shape[-1]).T[:16]
        rows_ref[...] = vecs
        for part in halves:
            recv(part.z[2])
            start(part.first[3])
        start(seg1.first, seg0.second[0], seg0.core[0])
        for k in range(4):
            part = slice(k * width, (k + 1) * width)
            bqv_ref[k, 0:1, :width] = vecs[3:4, part]
            bqv_ref[k, 0:1, width : 2 * width] = jnp.zeros((1, width), F32)
            bqv_ref[k, 0:1, 2 * width :] = vecs[4:5, part]
        fetch.wait()

        @pl.loop(0, n // step)
        def _(b):
            rows = pl.ds(pl.multiple_of(b * step, step), step)
            wide = x_ref[rows, :].astype(F32)
            xhat, _ = norm_parts(wide)
            a1 = (xhat * rows_ref[0:1, :] + rows_ref[2:3, :]).astype(BF16)
            a1_ref[rows, :] = a1
            a1t_ref[:, rows] = a1.T
            h1_ref[rows, :] = wide + rows_ref[5:6, :]

        put_a1t.start()
        start(seg2.z[0], seg1.z[1], seg1.z[0])
        recv(halves[0].first, halves[1].first)
        start(seg0.second[1], seg0.core[1])

    serve([0])

    @pl.when(h == 0)
    def _():
        here = all0_ref[t].reshape(D, 4 * width)
        gq = here[:, : 3 * width]
        gq_ref[0] = gq
        gw_ref[0] = here[:, 3 * width :]
        mine = place.group(t)
        qkv = dot_nn(a1_ref[...], gq) + bqv_ref[mine, 0:1, :]
        q = qkv[:, :width].astype(BF16) * jnp.asarray(HEAD_DIM ** -0.5, BF16)
        k = qkv[:, width : 2 * width].astype(BF16)
        v = qkv[:, 2 * width :].astype(BF16)
        q_ref[0] = q
        kt_ref[0] = k.T
        v_ref[0] = v
        vt = v.T
        for h in range(heads):
            vt_ref[h, :HEAD_DIM, :] = vt[h * HEAD_DIM : (h + 1) * HEAD_DIM]
        spare = k_ref.shape[1] - width
        dead = lax.broadcasted_iota(jnp.int32, (n, spare), 0) >= length
        first_column = lax.broadcasted_iota(jnp.int32, (n, spare), 1) == 0
        k_ref[:, :width] = k
        k_ref[:, width:] = jnp.where(first_column & dead, MASKED, 0.0).astype(BF16)
        qa_ref[:, :width] = q
        qa_ref[:, width:] = jnp.where(first_column, 1.0, 0.0).astype(BF16)
        scale_ref[0, heads:, :] = jnp.zeros((scale_ref.shape[1] - heads, n), F32)

    serve([1])

    lane = lax.broadcasted_iota(jnp.int32, (1, qa_ref.shape[1]), 1)
    keep = ((lane >= h * HEAD_DIM) & (lane < (h + 1) * HEAD_DIM)) | (lane >= width)
    key = lax.broadcasted_iota(jnp.int32, (step, step), 0)
    query = lax.broadcasted_iota(jnp.int32, (step, step), 1)
    head = pl.ds(pl.multiple_of(h * HEAD_DIM, HEAD_DIM), HEAD_DIM)

    def scores(b):
        first, last = b * step, (b + 1) * step
        q = jnp.where(keep, qa_ref[first:last, :], jnp.zeros((), BF16))
        return dot_nt(k_ref[:last, :], q)

    def attend(b, s):
        first, last = b * step, (b + 1) * step
        near = jnp.where(key <= query, s[first:], MASKED)
        top = jnp.max(near, 0, keepdims=True)
        if b:
            far = s[:first]
            top = jnp.maximum(top, jnp.max(far, 0, keepdims=True))
        e_near = jnp.exp((near - top).astype(BF16))
        p_ref[0, 0, b, first:last, :] = e_near
        o = dot_nn(vt_ref[h, :, first:last], e_near)
        if b:
            e_far = jnp.exp((far - top).astype(BF16))
            p_ref[0, 0, b, :first, :] = e_far
            o += dot_nn(vt_ref[h, :, :first], e_far)
        scale = 1.0 / o[HEAD_DIM : HEAD_DIM + 1]
        scale_ref[0, pl.ds(h, 1), first:last] = scale
        ot_ref[head, first:last] = (o[:HEAD_DIM] * scale).astype(BF16)

    s = scores(0)
    for b in range(n // step):
        ahead = scores(b + 1) if b + 1 < n // step else None
        attend(b, s)
        s = ahead

    serve([2, 3, 4])

    @pl.when(h == heads - 1)
    def _():
        o = ot_ref[...].T
        o_ref[0] = o
        h1_ref[...] += dot_nt(o, gw_ref[0])

    @pl.when((t == 3) & (h == heads - 1))
    def _():
        for i, rows in enumerate(blocks(n, step)):
            xhat, _ = norm_parts(h1_ref[rows, :])
            a2 = (xhat * rows_ref[1:2, :] + rows_ref[6:7, :]).astype(BF16)
            a2_ref[rows, :] = a2
            a2t_ref[:, rows] = a2.T
            for put in puts[i]:
                put.start()
        put_a2t.start()
        recv(seg2.core)
        flush[1][1].start()
        recv(seg1.core)
        flush[0][1].start()
        pass_second(seg1)
        flush[0][2].start()
        links.sent()
        for copies in flush + puts + [[put_a1t, put_a2t]]:
            for copy in copies:
                copy.wait()


N_GATHER = 10 + 14 + 6 + 10 + 10
VMEM_WHOLE = pl.BlockSpec(memory_space=pltpu.VMEM)
ANY_WHOLE = pl.BlockSpec(memory_space=pl.ANY)


def run_fused_forward(tie, lengths, tokens, gains, biases, w_in, w_out, w_expand, w_project):
    groups, n, _ = tokens.shape
    depth, width = w_in.shape[-2:]
    heads = width // HEAD_DIM
    hidden = w_expand.shape[-1]
    w_project = w_project.transpose(0, 2, 1)
    biases = biases.transpose(1, 0, 2)
    own = gains.shape[-1]

    def group(*shape):
        return pl.BlockSpec((1,) + shape, lambda t, h: (t,) + (0,) * len(shape))

    per_head = pl.BlockSpec((1, 1, n // 256, n, 256), lambda t, h: (t, h, 0, 0, 0))
    return pl.pallas_call(
        fused_forward,
        grid=(groups, heads),
        in_specs=[SMEM_WHOLE, SMEM_WHOLE, ANY_WHOLE] + [VMEM_WHOLE] * 6,
        out_specs=[
            group(D, 3 * width), group(D, width), ANY_WHOLE, ANY_WHOLE, VMEM_WHOLE,
            group(n, width), group(n, width), group(width, n), per_head,
            group(8, n), group(n, width), ANY_WHOLE, ANY_WHOLE, ANY_WHOLE, ANY_WHOLE,
        ],
        out_shape=[
            shaped(BF16, groups, D, 3 * width), shaped(BF16, groups, D, width),
            shaped(BF16, groups, Z_DEV, Y_DEV, depth, hidden),
            shaped(BF16, groups, Z_DEV, Y_DEV, depth, hidden),
            shaped(F32, 16, D),
            shaped(BF16, groups, n, width), shaped(BF16, groups, n, width),
            shaped(BF16, groups, width, n), shaped(BF16, groups, heads, n // 256, n, 256),
            shaped(F32, groups, 8, n), shaped(BF16, groups, n, width), shaped(BF16, D, n), shaped(F32, n, D),
            shaped(BF16, n, D), shaped(BF16, D, n),
        ],
        scratch_shapes=[
            pltpu.VMEM((depth, 4 * width), BF16),
            pltpu.VMEM((depth, hidden), BF16), pltpu.VMEM((depth, hidden), BF16),
            pltpu.VMEM((128, 128), F32), pltpu.VMEM((own, 128), F32),
            pltpu.VMEM((groups, Z_DEV, Y_DEV, depth, 4 * width), BF16),
            pltpu.VMEM((groups, Z_DEV, Y_DEV, depth, hidden), BF16),
            pltpu.VMEM((groups, Z_DEV, Y_DEV, depth, hidden), BF16),
            pltpu.VMEM((Z_DEV, Y_DEV, X_DEV, C_DEV, own, 128), F32),
            pltpu.VMEM((groups, 8, 3 * width), F32),
            pltpu.VMEM((n, D), BF16), pltpu.VMEM((n, D), BF16), pltpu.VMEM((n, 256), BF16),
            pltpu.VMEM((n, 256), BF16), pltpu.VMEM((heads, HEAD_DIM + 16, n), BF16),
            pltpu.VMEM((width, n), BF16),
            pltpu.VMEM((D, n), BF16), pltpu.VMEM((n, D), F32), pltpu.VMEM((n, D), BF16),
            pltpu.VMEM((D, n), BF16),
            pltpu.SemaphoreType.DMA((N_GATHER,)), pltpu.SemaphoreType.DMA((N_GATHER,)),
            pltpu.SemaphoreType.DMA((3,)), pltpu.SemaphoreType.DMA((2, 4)),
            pltpu.SemaphoreType.DMA((2, n // 256)),
        ],
        compiler_params=pltpu.CompilerParams(
            vmem_limit_bytes=VMEM_LIMIT, collective_id=0, has_side_effects=True
        ),
        name="fused_forward",
    )(tie, lengths, tokens, gains, biases, w_in, w_out, w_expand, w_project)


class Result:
    def __init__(self, links, place, own_ref, passing_ref, out_ref, step, sem, count):
        self.x, self.core, self.far, self.keep, self.keep_far = [], [], [], [], []
        for i in range(count):
            rows = pl.ds(i * step, step)
            mine, theirs = out_ref.at[place.t, rows], out_ref.at[place.ts[2], rows]
            own, passing = own_ref.at[rows], passing_ref.at[rows]
            self.x.append(links.add(place.to_x, own, passing))
            self.core.append(links.add(place.to_core, own, mine))
            self.far.append(links.add(place.to_core, passing, theirs))
            self.keep.append(pltpu.make_async_copy(own, mine, sem.at[0, i]))
            self.keep_far.append(pltpu.make_async_copy(passing, theirs, sem.at[1, i]))

    def send(self, i):
        start(self.x[i], self.core[i], self.keep[i])

    def pass_on(self, i):
        recv(self.x[i])
        start(self.far[i], self.keep_far[i])

    def finish(self):
        recv(self.core, self.far)
        for copy in self.keep + self.keep_far:
            copy.wait()


def low(value):
    return jnp.asarray(value, BF16)


def pair_order(i):
    return i + 1 - 2 * (i % 2)


def fused_feed_forward(
    len_ref, cot_ref, a2_ref, a2t_in, h1_in, far1_ref, far2_ref, rows_ref,
    out_out, fold_ref, work_out, dh1_out, gb_out, gbt_out, sums_ref,
    gf_ref, gft_ref, feed_ref, da2_ref, h_ref, df_ref, weights_ref, missing_ref, third_ref,
    stage_ref, land_ref, near_ref, cross_ref, a2t_ref, h1_ref, out_ref, work_ref,
    send_sem, recv_sem, local_sem, row_sem,
):
    t = pl.program_id(0)
    n = gf_ref.shape[0]
    step = 256
    depth = stage_ref.shape[-2]
    place = Place()
    length = len_ref[place.t]
    links = Links(send_sem, recv_sem)
    y, other = place.y, place.other_y
    last = [
        links.add(place.to_x, far1_ref.at[0, :, other], missing_ref.at[0, 0]),
        links.add(place.to_y, far2_ref.at[2, :, y], missing_ref.at[1, 0]),
    ]
    last_core = [
        links.add(place.to_core, missing_ref.at[i, 0], missing_ref.at[i, 1]) for i in range(2)
    ]
    third = [
        links.add(place.to_core, far_ref.at[2, :, y], third_ref.at[i])
        for i, far_ref in enumerate([far1_ref, far2_ref])
    ]
    core = [
        [links.add(place.to_core, stage_ref.at[i], land_ref.at[s, i]) for i in range(2)]
        for s in range(2)
    ]
    cross = [
        links.add(place.to_y, near_ref.at[i, :, other], cross_ref.at[i]) for i in range(2)
    ]
    fetch = pltpu.make_async_copy(cot_ref.at[place.t], gf_ref, local_sem.at[0])
    gb_ref, gbt_ref, dh1_ref = gf_ref, gft_ref, da2_ref
    late = [
        pltpu.make_async_copy(a2t_in, a2t_ref, local_sem.at[5]),
        pltpu.make_async_copy(h1_in, h1_ref, local_sem.at[6]),
    ]
    puts = []
    for i in range(n // step):
        rows = pl.ds(i * step, step)
        puts.append([
            pltpu.make_async_copy(ref.at[rows], out.at[rows], row_sem.at[j, i])
            for j, (ref, out) in enumerate(
                [(out_ref, out_out), (dh1_ref, dh1_out), (gb_ref, gb_out)]
            )
        ])
    put_gbt = pltpu.make_async_copy(gbt_ref, gbt_out, local_sem.at[7])
    put_work = pltpu.make_async_copy(work_ref, work_out, local_sem.at[8])
    k = pair_order(t)
    mine = place.group(k)

    def load(step, whole, slot):
        for i, far_ref in enumerate([far1_ref, far2_ref]):
            group = far_ref.at[pair_order(step)]
            to = weights_ref.at[slot, i]
            if not whole:
                group, to = group.at[:, y], to.at[:, y]
            yield pltpu.make_async_copy(group, to, local_sem.at[1 + 2 * slot + i])

    def live_rows(b):
        at = b * step + lax.broadcasted_iota(jnp.int32, (step, 1), 0)
        return (at < length).astype(F32)

    @pl.when(t == 0)
    def _():
        fetch.start()
        for copy in load(0, True, 0):
            copy.start()
        for copy in late:
            copy.start()
        place.greet()
        start(last, third)
        sums_ref[...] = jnp.zeros_like(sums_ref)
        feed_ref[...] = jnp.zeros_like(feed_ref)
        da2_ref[...] = jnp.zeros_like(da2_ref)
        fetch.wait()

        @pl.loop(0, n // step)
        def _(b):
            rows = pl.ds(pl.multiple_of(b * step, step), step)
            g = (gf_ref[rows, :].astype(F32) * live_rows(b)).astype(BF16)
            gf_ref[rows, :] = g
            gft_ref[:, rows] = g.T
            sums_ref[7:8, :] += jnp.sum(g.astype(F32), 0, keepdims=True)

    for i in range(4):
        @pl.when(t == i)
        def _():
            if i == 2:
                recv(last_core, third)
            else:
                for copy in load(i, i < 2, i % 2):
                    copy.wait()
            if i in (0, 2):
                for copy in load(i + 1, i + 1 < 2, (i + 1) % 2):
                    copy.start()
            for j in range(2):
                if i == 2:
                    weights_ref[0, j, :, y] = third_ref[j]
                if i >= 2:
                    weights_ref[i % 2, j, :, other] = missing_ref[j, 3 - i]

    bias = rows_ref[pl.ds(8 + mine, 1), :]
    w1 = weights_ref[t % 2, 0].reshape(D, -1)
    w2 = weights_ref[t % 2, 1].reshape(D, -1)
    column = jnp.zeros((1, w1.shape[1]), F32)
    for rows in blocks(n, step):
        f = (dot_nn(a2_ref[rows, :], w1) + bias).astype(BF16)
        dh = dot_nn(gf_ref[rows, :], w2)
        f2 = f * f
        th = jnp.tanh(f * (low(SQRT_2_PI) + low(SQRT_2_PI * 0.044715) * f2))
        half = low(0.5) + low(0.5) * th
        h = f * half
        slope = half + f * (low(0.5) - low(0.5) * th * th) * (
            low(SQRT_2_PI) + low(3 * SQRT_2_PI * 0.044715) * f2
        )
        df = (dh * slope.astype(F32)).astype(BF16)
        h_ref[rows, :] = h
        df_ref[rows, :] = df
        column += jnp.sum(df.astype(F32), 0, keepdims=True)
        feed_ref[rows, :] += dot_nt(h, w2)
        da2_ref[rows, :] += dot_nt(df, w1)
    sums_ref[pl.ds(8 + mine, 1), :] = column

    @pl.when(t == 1)
    def _():
        recv(last)
        start(last_core)

    @pl.when(t == 0)
    def _():
        late[0].wait()

    def weight_grad(left_ref, right_ref):
        value = dot_nn(left_ref[...], right_ref[...])
        return value.reshape(Z_DEV, Y_DEV, depth, value.shape[-1]).astype(BF16)

    grad1 = weight_grad(a2t_ref, df_ref)
    grad2 = weight_grad(gft_ref, h_ref)

    def put(ref):
        ref[0] = grad1
        ref[1] = grad2

    def reduced(ref):
        return lambda i, s, z: (
            ref[i, z].astype(F32) + land_ref[s, i, z].astype(F32)
        ).astype(BF16)

    @pl.when(t == 0)
    def _():
        put(stage_ref)
        start(core[0])

    @pl.when(t == 1)
    def _():
        put(near_ref)
        recv(core[0])

        @pl.loop(0, Z_DEV)
        def _(z):
            for i in range(2):
                near_ref[i, z] = reduced(near_ref)(i, 0, z)

        start(cross)

    @pl.when(t == 2)
    def _():
        for copy in core[0]:
            copy.wait_send()
        put(stage_ref)
        start(core[1])

    @pl.when(t == 3)
    def _():
        put(work_ref)
        late[1].wait()
        for i, rows in enumerate(blocks(n, step)):
            live = live_rows(i)
            h1 = h1_ref[rows, :]
            out_ref[rows, :] = (live * (h1 + (feed_ref[rows, :] + rows_ref[7:8, :]))).astype(BF16)
            xhat, r = norm_parts(h1)
            da2 = da2_ref[rows, :]
            sums_ref[1:2, :] += jnp.sum(da2 * xhat, 0, keepdims=True)
            sums_ref[6:7, :] += jnp.sum(da2, 0, keepdims=True)
            dg = da2 * rows_ref[1:2, :]
            dv = r * (
                dg
                - jnp.mean(dg, -1, keepdims=True)
                - xhat * jnp.mean(dg * xhat, -1, keepdims=True)
            )
            dh1 = gf_ref[rows, :].astype(F32) + dv
            dh1_ref[rows, :] = dh1
            gb = dh1.astype(BF16)
            gb_ref[rows, :] = gb
            gbt_ref[:, rows] = gb.T
            sums_ref[5:6, :] += jnp.sum(gb.astype(F32), 0, keepdims=True)
            for copy in puts[i]:
                copy.start()
        put_gbt.start()
        recv(core[1])

        @pl.loop(0, Z_DEV)
        def _(z):
            for i in range(2):
                work_ref[i, z] = reduced(work_ref)(i, 1, z)

        put_work.start()
        recv(cross)

        @pl.loop(0, Z_DEV)
        def _(z):
            for i in range(2):
                fold_ref[i, z] = (
                    near_ref[i, z, y].astype(F32) + cross_ref[i, z].astype(F32)
                ).astype(BF16)

        links.sent(*core[0])
        for copies in puts + [[put_gbt, put_work]]:
            for copy in copies:
                copy.wait()


def run_fused_feed_forward(lengths, cot, a2, a2t, h1, g1, g2, rows):
    n = cot.shape[1]
    groups, _, _, depth, hidden = g1.shape
    both = (2, Z_DEV, Y_DEV, depth, hidden)
    fold = (2, Z_DEV, depth, hidden)
    return pl.pallas_call(
        fused_feed_forward,
        grid=(groups,),
        in_specs=[SMEM_WHOLE, ANY_WHOLE, VMEM_WHOLE] + [ANY_WHOLE] * 4 + [VMEM_WHOLE],
        out_specs=[ANY_WHOLE, VMEM_WHOLE] + [ANY_WHOLE] * 4 + [VMEM_WHOLE],
        out_shape=[
            shaped(BF16, n, D), shaped(BF16, *fold), shaped(BF16, *both), shaped(F32, n, D),
            shaped(BF16, n, D), shaped(BF16, D, n), shaped(F32, 16, D),
        ],
        scratch_shapes=[
            pltpu.VMEM((n, D), BF16), pltpu.VMEM((D, n), BF16), pltpu.VMEM((n, D), F32),
            pltpu.VMEM((n, D), F32), pltpu.VMEM((n, hidden), BF16), pltpu.VMEM((n, hidden), BF16),
            pltpu.VMEM((2,) + both, BF16),
            pltpu.VMEM((2,) + fold, BF16), pltpu.VMEM(fold, BF16), pltpu.VMEM(both, BF16),
            pltpu.VMEM((2,) + both, BF16),
            pltpu.VMEM(both, BF16), pltpu.VMEM(fold, BF16),
            pltpu.VMEM((D, n), BF16), pltpu.VMEM((n, D), F32), pltpu.VMEM((n, D), BF16),
            pltpu.VMEM(both, BF16),
            pltpu.SemaphoreType.DMA((12,)), pltpu.SemaphoreType.DMA((12,)),
            pltpu.SemaphoreType.DMA((9,)), pltpu.SemaphoreType.DMA((3, n // 256)),
        ],
        compiler_params=pltpu.CompilerParams(
            vmem_limit_bytes=VMEM_LIMIT, collective_id=1, has_side_effects=True
        ),
        name="fused_feed_forward",
    )(lengths, cot, a2, a2t, h1, g1, g2, rows)
class Reduce:
    def __init__(
        self, links, place, work, acc, cross_ref, far_ref, mid_ref, last_ref, side_ref,
        slots=(0, 1),
    ):
        self.place, self.work, self.acc = place, work, acc
        self.cross_ref, self.far_ref, self.mid_ref = cross_ref, far_ref, mid_ref
        self.last_ref, self.side_ref = last_ref, side_ref
        self.two = len(slots) == 2
        zs = place.zs
        self.y = {
            s: [
                links.add(
                    place.to_y, work(s, zs[j], place.other_y),
                    cross_ref.at[s if self.two else 0, zs[j]],
                )
                for j in (1, 3, 2, 0)
            ]
            for s in slots
        }
        self.z = [
            [
                links.add(place.to_z[1], acc(s, zs[1]), far_ref.at[s, 0]),
                links.add(place.to_z[1], acc(s, zs[3]), far_ref.at[s, 1]),
                links.add(place.to_z[2], mid_ref.at[s, 1], far_ref.at[s, 2]),
            ]
            for s in range(2)
        ]
        self.x = links.add(place.to_x, last_ref, side_ref)

    def fold_y(self, s, half):
        for i, j in [(0, 1), (1, 3), (2, 2), (3, 0)][2 * half : 2 * half + 2]:
            z = self.place.zs[j]
            recv(self.y[s][i])
            value = self.work(s, z, self.place.y)[...].astype(F32)
            cross = self.cross_ref[s if self.two else 0, z].astype(F32)
            self.acc(s, z)[...] = (value + cross).astype(BF16)
            if i < 2:
                start(self.z[s][i])

    def fold_z(self, s):
        recv(self.z[s][:2])
        for i in (1, 0):
            value = self.acc(s, self.place.zs[2 * i])[...].astype(F32)
            self.mid_ref[s, i] = (value + self.far_ref[s, i].astype(F32)).astype(BF16)
            if i:
                start(self.z[s][2])

    def own(self, s):
        recv(self.z[s][2])
        return self.mid_ref[s, 0].astype(F32) + self.far_ref[s, 2].astype(F32)

    def send_x(self):
        self.last_ref[...] = self.own(1).astype(BF16)
        start(self.x)

    def total(self):
        value = self.own(0)
        recv(self.x)
        return value + self.side_ref[...].astype(F32)


def fused_backward(
    tokens_ref, gq_in, gw_in, rows_ref, dh1_ref, gb_ref, gbt_in, q_in, v_in, kt_in,
    p_ref, scale_in, o_in, a1t_in, layer_in, fold_in, work_in, early_ref,
    out_ref, layerout_ref, part0_ref, part1_ref, part2_ref, total_ref,
    gq_ref, gw_ref, q_ref, v_ref, kt_ref, scale_ref, o_ref,
    a1t_ref, gbt_ref, layer_ref, fold_ref, work_ref, do_ref, delta_ref, dkv_ref, dqkv_ref, hold_ref, da1_ref, own_ref, passing_ref, passlayer_ref, bqv_ref,
    folded_ref, cross1_ref, far1_ref, mid1_ref, last1_ref, side1_ref,
    cross2_ref, far2_ref, mid2_ref, last2_ref, side2_ref,
    stage0_ref, land0_ref, work0_ref, cross0_ref, far0_ref, mid0_ref, last0_ref, side0_ref,
    sums_ref, sumland_ref,
    send_sem, recv_sem, local_sem, result_sem, group_sem,
):
    t = pl.program_id(0)
    n = own_ref.shape[0]
    width = gw_ref.shape[-1]
    depth = part0_ref.shape[0]
    heads = width // HEAD_DIM
    step = n // 4
    place = Place()
    y = place.y
    links = Links(send_sem, recv_sem)
    k, i = group_and_block(t)
    mine = place.group(k)
    now = k % 2
    out = Result(links, place, own_ref, passing_ref, out_ref, step, result_sem.at[0], 4)
    layer = Result(links, place, layer_ref, passlayer_ref, layerout_ref, step, result_sem.at[1], 4)
    fetch = pltpu.make_async_copy(tokens_ref.at[place.t], own_ref, local_sem.at[0])
    fetch_layer, fetch_work, fetch_fold, fetch_gbt, fetch_a1t = [
        pltpu.make_async_copy(there, here, local_sem.at[1 + j])
        for j, (there, here) in enumerate([
            (layer_in, layer_ref), (work_in, work_ref), (fold_in, fold_ref),
            (gbt_in, gbt_ref), (a1t_in, a1t_ref),
        ])
    ]
    def operands(group):
        slot = group % 2
        pairs = [
            (gw_in, gw_ref), (scale_in, scale_ref), (o_in, o_ref), (v_in, v_ref),
            (q_in, q_ref), (kt_in, kt_ref), (gq_in, gq_ref),
        ]
        return [
            pltpu.make_async_copy(there.at[group], here.at[slot], group_sem.at[slot, j])
            for j, (there, here) in enumerate(pairs)
        ]

    core0 = [links.add(place.to_core, stage0_ref, land0_ref.at[i]) for i in range(2)]
    def half_done(i, *landing):
        return Reduce(
            links, place, lambda s, z, y: work_ref.at[i, z, y],
            lambda s, z: folded_ref.at[i, z] if s else fold_ref.at[i, z],
            *landing, slots=(1,),
        )

    seg1 = half_done(0, cross1_ref, far1_ref, mid1_ref, last1_ref, side1_ref)
    seg2 = half_done(1, cross2_ref, far2_ref, mid2_ref, last2_ref, side2_ref)
    seg0 = Reduce(
        links, place, lambda s, z, y: work0_ref.at[s, z, y],
        lambda s, z: work0_ref.at[s, z, y],
        cross0_ref, far0_ref, mid0_ref, last0_ref, side0_ref,
    )
    sum_core, sum_y, *sum_z, sum_x = [
        links.add(to, sums_ref.at[i], sumland_ref.at[j])
        for j, (i, to) in enumerate(
            zip([0, 1, 2, 2, 2, 3], [place.to_core, place.to_y] + place.to_z[1:] + [place.to_x])
        )
    ]

    def when(point):
        return pl.when(t == point)

    @when(0)
    def _():
        start(fetch_layer, operands(1), fetch_work, fetch_fold, fetch_gbt, operands(0))
        start(fetch, fetch_a1t)
        place.greet()
        fetch_layer.wait()
        for i in range(4):
            layer.send(i)
        fetch_work.wait()
        start(seg1.y[1], seg2.y[1])
        fetch_fold.wait()
        start(seg1.z[0][:2], seg2.z[0][:2])
        bqv_ref[...] = jnp.zeros_like(bqv_ref)
        sums_ref[0] = early_ref[...]
        fetch_gbt.wait()

    def wait(copies):
        for copy in copies:
            copy.wait()

    @when(0)
    def _():
        wait(operands(1))

    @when(4)
    def _():
        start(operands(3))
        wait(operands(0))

    @when(8)
    def _():
        start(operands(2))
        wait(operands(3))

    @when(9)
    def _():
        wait(operands(2))

    plan = [
        (2, 1, lambda: (seg1.fold_y(1, 0), seg1.fold_z(0))),
        (3, 1, lambda: layer.pass_on(0)),
        (4, 0, lambda: (seg1.fold_y(1, 1), seg2.fold_z(0))),
        (4, 1, lambda: layer.pass_on(1)),
        (5, 1, lambda: (seg1.fold_z(1), seg2.fold_y(1, 0))),
        (8, 0, lambda: (seg2.fold_y(1, 1), layer.pass_on(2))),
        (8, 1, lambda: seg1.send_x()),
        (9, 1, lambda: (seg2.fold_z(1), seg0.fold_y(0, 0), layer.pass_on(3))),
        (11, 1, lambda: (seg2.send_x(), seg0.fold_y(0, 1))),
        (13, 1, lambda: (seg0.fold_z(0), out.pass_on(3))),
    ]

    def serve(point):
        for at, where, act in plan:
            if where == point:
                pl.when(t == at)(lambda act=act: (act(), None)[1])

    @pl.when((t == 0) | (t == 4) | (t == 8) | (t == 9))
    def _():
        pick = (
            lax.broadcasted_iota(jnp.int32, (8, width), 1) // HEAD_DIM
            == lax.broadcasted_iota(jnp.int32, (8, width), 0)
        ).astype(BF16)

        @pl.loop(0, n // step)
        def _(i):
            rows = pl.ds(pl.multiple_of(i * step, step), step)
            columns = scale_ref[now, :, rows].T
            lane = lax.broadcasted_iota(jnp.int32, (step, width), 1)
            scale = columns[:, heads - 1 : heads]
            for h in reversed(range(heads - 1)):
                scale = jnp.where(lane < (h + 1) * HEAD_DIM, columns[:, h : h + 1], scale)
            do = (dot_nn(gb_ref[rows, :], gw_ref[now]) * scale).astype(BF16)
            do_ref[now, rows, :] = do
            product = do.astype(F32) * o_ref[now, rows, :].astype(F32)
            high = product.astype(BF16)
            low = (product - high.astype(F32)).astype(BF16)
            delta_ref[now, :, rows] = dot_nt(pick, high) + dot_nt(pick, low)

        value = dot_nn(gbt_ref[...], o_ref[now]).astype(BF16)
        value = value.reshape(Z_DEV, Y_DEV, depth, width)

        hold_ref[now] = value

    serve(0)

    for ii in reversed(range(4)):
        @pl.when(i == ii)
        def _():
            first, last = ii * step, (ii + 1) * step
            do = do_ref[now, first:last, :]
            q = q_ref[now, first:last, :]
            v = v_ref[now, :last, :]
            lane = lax.broadcasted_iota(jnp.int32, (1, width), 1)
            heads_of = [
                (lane >= h * HEAD_DIM) & (lane < (h + 1) * HEAD_DIM) for h in range(heads)
            ]
            zero = jnp.zeros((), BF16)

            def stacked(ref):
                return ref.reshape(heads * last, ref.shape[-1])

            def picked(value):
                out = value[:last]
                for h in range(1, heads):
                    out = jnp.where(heads_of[h], value[h * last : (h + 1) * last], out)
                return out

            p = p_ref[0, :, 0, :last, :]
            dp = dot_nt(jnp.concatenate([jnp.where(m, v, zero) for m in heads_of], 0), do)
            delta = delta_ref[now, :heads, first:last]
            ds = p * (dp.reshape(heads, last, step) - delta[:, None, :]).astype(BF16)
            dk = picked(dot_nn(stacked(ds), q))
            dv = picked(dot_nn(stacked(p), do))
            dq = [
                dot_nn(kt_ref[now, h * HEAD_DIM : (h + 1) * HEAD_DIM, :last], ds[h])
                for h in range(heads)
            ]
            if ii == 3:
                dkv_ref[now, 0] = dk
                dkv_ref[now, 1] = dv
            else:
                dkv_ref[now, 0, :last, :] += dk
                dkv_ref[now, 1, :last, :] += dv
            dk = dkv_ref[now, 0, first:last, :].astype(BF16)
            dv = dkv_ref[now, 1, first:last, :].astype(BF16)
            dq = (jnp.concatenate(dq, 0) * HEAD_DIM ** -0.5).astype(BF16).T
            dqkv_ref[now, first:last, :width] = dq
            dqkv_ref[now, first:last, width : 2 * width] = dk
            dqkv_ref[now, first:last, 2 * width :] = dv
            bqv_ref[mine, 0:1, :] += jnp.sum(dq.astype(F32), 0, keepdims=True)
            bqv_ref[mine, 1:2, :] += jnp.sum(dv.astype(F32), 0, keepdims=True)

            @pl.when(t >= 8)
            def _():
                da1_ref[first:last, :] += dot_nt(dqkv_ref[now, first:last, :], gq_ref[now])

    serve(1)

    @pl.when((t == 3) | (t == 7) | (t > 13))
    def _():
        @when(3)
        def _():
            fetch.wait()
            fetch_a1t.wait()

        @when(3)
        def _():
            da1_ref[...] = dot_nt(dqkv_ref[now], gq_ref[now])

        @when(7)
        def _():
            da1_ref[...] += dot_nt(dqkv_ref[now], gq_ref[now])

        value = dot_nn(a1t_ref[...], dqkv_ref[now]).reshape(Z_DEV, Y_DEV, depth, 3 * width)
        value = jnp.concatenate([value, hold_ref[now].astype(F32)], -1)
        for s in range(2):
            @when(3 + 11 * s)
            def _():
                if s:
                    core0[0].wait_send()
                stage0_ref[...] = value.astype(BF16)
                start(core0[s])

            @when(7 + 8 * s)
            def _():
                recv(core0[s])
                work0_ref[s] = (value + land0_ref[s].astype(F32)).astype(BF16)
                start(seg0.y[s])

    @pl.when((t > 8) & (t % 2 == 1))
    def _():
        rows = pl.ds(pl.multiple_of(i * step, step), step)
        xhat, r = norm_parts(own_ref[rows, :].astype(F32))
        da1 = da1_ref[rows, :]
        sums_ref[0, 0:1, :] += jnp.sum(da1 * xhat, 0, keepdims=True)
        sums_ref[0, 2:3, :] += jnp.sum(da1, 0, keepdims=True)
        dg = da1 * rows_ref[0:1, :]
        dv = r * (
            dg
            - jnp.mean(dg, -1, keepdims=True)
            - xhat * jnp.mean(dg * xhat, -1, keepdims=True)
        )
        own_ref[rows, :] = (dh1_ref[...] + dv).astype(BF16)
        for ii in range(4):
            @pl.when(i == ii)
            def _():
                out.send(ii)

    @when(15)
    def _():
        for s in range(4):
            sums_ref[0, 3:5, s * width : (s + 1) * width] = bqv_ref[s, 0:2, :]
        start(sum_core)
        out.pass_on(2)
        recv(sum_core)
        sums_ref[1] = sums_ref[0] + sumland_ref[0]
        start(sum_y)
        seg0.fold_y(1, 0)
        out.pass_on(1)
        seg0.fold_y(1, 1)
        recv(sum_y)
        sums_ref[2] = sums_ref[1] + sumland_ref[1]
        start(sum_z)
        seg0.fold_z(1)
        recv(sum_z)
        sums_ref[3] = (sums_ref[2] + sumland_ref[2]) + (sumland_ref[3] + sumland_ref[4])
        start(sum_x)
        part1_ref[...] = seg1.total()
        part2_ref[...] = seg2.total()
        seg0.send_x()
        layer.finish()
        out.pass_on(0)
        recv(sum_x)
        total_ref[...] = sums_ref[3] + sumland_ref[5]
        part0_ref[...] = seg0.total()
        out.finish()
        links.sent(core0[0])


def group_and_block(t):
    early = t < 8
    return (
        jnp.where(early, 1 - t // 4, 3 - t % 2),
        3 - jnp.where(early, t % 4, jnp.maximum(t - 8, 0) // 2),
    )


def run_fused_backward(
    tokens, gq, gw, rows, dh1, gb, gbt, q, v, kt, p, scale, o, a1t, layer, fold, work, early
):
    groups, n, _ = tokens.shape
    width = gw.shape[-1]
    heads = width // HEAD_DIM
    hidden = fold.shape[-1]
    depth = D // (Z_DEV * Y_DEV)
    step = n // 4

    p_spec = pl.BlockSpec(
        (1, heads, 1, n, step),
        lambda t: (group_and_block(t)[0], 0, group_and_block(t)[1], 0, 0),
    )

    copies = 2 * 12 + 2 + 15 + 2 * 11 + 6

    def landing(lanes, slots=1):
        return [
            pltpu.VMEM((slots, Z_DEV, depth, lanes), BF16),
            pltpu.VMEM((2, 3, depth, lanes), BF16), pltpu.VMEM((2, 2, depth, lanes), BF16),
            pltpu.VMEM((depth, lanes), BF16), pltpu.VMEM((depth, lanes), BF16),
        ]

    def working(lanes):
        block = (Z_DEV, Y_DEV, depth, lanes)
        return [pltpu.VMEM(block, BF16)] + [pltpu.VMEM((2,) + block, BF16)] * 2

    return pl.pallas_call(
        fused_backward,
        grid=(4 * groups,),
        in_specs=[
            ANY_WHOLE, ANY_WHOLE, ANY_WHOLE, VMEM_WHOLE,
            pl.BlockSpec((step, D), lambda t: (group_and_block(jnp.maximum(t, 8))[1], 0)),
            VMEM_WHOLE, ANY_WHOLE, ANY_WHOLE, ANY_WHOLE, ANY_WHOLE, p_spec,
            ANY_WHOLE, ANY_WHOLE, ANY_WHOLE, ANY_WHOLE, ANY_WHOLE, ANY_WHOLE, VMEM_WHOLE,
        ],
        out_specs=[ANY_WHOLE] * 2 + [VMEM_WHOLE] * 4,
        out_shape=[
            shaped(BF16, groups, n, D), shaped(BF16, groups, n, D),
            shaped(F32, depth, 4 * width), shaped(F32, depth, hidden),
            shaped(F32, depth, hidden), shaped(F32, 16, D),
        ],
        scratch_shapes=[
            pltpu.VMEM((2, D, 3 * width), BF16), pltpu.VMEM((2, D, width), BF16),
            pltpu.VMEM((2, n, width), BF16), pltpu.VMEM((2, n, width), BF16),
            pltpu.VMEM((2, width, n), BF16), pltpu.VMEM((2, 8, n), F32),
            pltpu.VMEM((2, n, width), BF16),
            pltpu.VMEM((D, n), BF16), pltpu.VMEM((D, n), BF16), pltpu.VMEM((n, D), BF16),
            pltpu.VMEM((2, Z_DEV, depth, hidden), BF16),
            pltpu.VMEM((2, Z_DEV, Y_DEV, depth, hidden), BF16),
            pltpu.VMEM((2, n, width), BF16),
            pltpu.VMEM((2, 8, n), F32), pltpu.VMEM((2, 2, n, width), F32),
            pltpu.VMEM((2, n, 3 * width), BF16),
            pltpu.VMEM((2, Z_DEV, Y_DEV, depth, width), BF16), pltpu.VMEM((n, D), F32),
            pltpu.VMEM((n, D), BF16), pltpu.VMEM((n, D), BF16), pltpu.VMEM((n, D), BF16),
            pltpu.VMEM((groups, 8, width), F32),
        ]
        + [pltpu.VMEM((2, Z_DEV, depth, hidden), BF16)] + landing(hidden) + landing(hidden)
        + working(4 * width) + landing(4 * width, 2)
        + [
            pltpu.VMEM((4, 16, D), F32), pltpu.VMEM((6, 16, D), F32),
            pltpu.SemaphoreType.DMA((copies,)), pltpu.SemaphoreType.DMA((copies,)),
            pltpu.SemaphoreType.DMA((6,)), pltpu.SemaphoreType.DMA((2, 2, 4)),
            pltpu.SemaphoreType.DMA((2, 7)),
        ],
        compiler_params=pltpu.CompilerParams(
            vmem_limit_bytes=VMEM_LIMIT, collective_id=2, has_side_effects=True
        ),
        name="fused_backward",
    )(tokens, gq, gw, rows, dh1, gb, gbt, q, v, kt, p, scale, o, a1t, layer, fold, work, early)


def place_gradients(
    tie_ref, sums_ref, part0_ref, part1_ref, part2_ref, near_out_ref,
    near_grad_ref, far_out_ref, far_grad_ref, gains_ref, bias_ref, in_ref, out_ref, expand_ref,
    project_ref, chosen_ref,
):
    t = pl.program_id(0)
    far_out_ref[...] = near_out_ref[...]
    far_grad_ref[...] = near_grad_ref[...]
    own = gains_ref.shape[-1]
    width = part0_ref.shape[-1] // 4
    kinds = [tie_ref[0], tie_ref[1], tie_ref[2], tie_ref[3]]

    @pl.when(t == 0)
    def _():
        first = (lax.axis_index("dp") * 4 + lax.axis_index("tensor")) * own
        feature = lax.broadcasted_iota(jnp.int32, (D, 128), 0)
        lane = lax.broadcasted_iota(jnp.int32, (D, 128), 1)
        chosen = ((feature == first + lane) & (lane < own)).astype(F32)
        chosen_ref[...] = lax.dot_general(
            sums_ref[...], chosen, (((1,), (0,)), ((), ())),
            precision=lax.Precision.HIGHEST, preferred_element_type=F32,
        )
        row = lax.broadcasted_iota(jnp.int32, (NSRC, own), 0)
        for i, kind in enumerate([0, 0, 0, 1, 2, 3, 2, 2, 2, 2]):
            value = chosen_ref[2 + i : 3 + i, :own]
            bias_ref[i] = jnp.where(row == kinds[kind], value, 0.0)

    @pl.when(t < NSRC)
    def _():
        def here(kind, value):
            return jnp.where(kinds[kind] == t, value, jnp.zeros_like(value))

        gains_ref[0, 0:1] = here(0, chosen_ref[0:1, :own])
        gains_ref[0, 1:2] = here(2, chosen_ref[1:2, :own])
        for j in range(3):
            in_ref[0, j] = here(0, part0_ref[:, j * width : (j + 1) * width])
        out_ref[0] = here(1, part0_ref[:, 3 * width :].T)
        expand_ref[0] = here(2, part1_ref[...])
        project_ref[0] = here(3, part2_ref[...])


def run_place_gradients(tie, sums, part0, part1, part2, out, grad, like):
    slots, n, _ = grad.shape
    gains, biases, w_in, w_out, w_expand, w_project = [item.shape for item in like]
    shapes = [
        gains, (biases[1], biases[0], biases[2]), w_in, w_out, w_expand,
        (w_project[0], w_project[2], w_project[1]),
    ]

    def source(shape):
        return pl.BlockSpec(
            (1,) + shape[1:], lambda t: (jnp.minimum(t, NSRC - 1),) + (0,) * (len(shape) - 1)
        )

    out, grad, gains, biases, w_in, w_out, w_expand, w_project = pl.pallas_call(
        place_gradients,
        grid=(slots,),
        in_specs=[SMEM_WHOLE] + [VMEM_WHOLE] * 4 + [group(n, D), group(n, D)],
        out_specs=[group(n, D), group(n, D), source(shapes[0]), VMEM_WHOLE]
        + [source(shape) for shape in shapes[2:]],
        out_shape=[shaped(BF16, slots, n, D)] * 2 + [shaped(F32, *item) for item in shapes],
        scratch_shapes=[pltpu.VMEM((16, 128), F32)],
        compiler_params=pltpu.CompilerParams(vmem_limit_bytes=VMEM_LIMIT),
        name="place_gradients",
    )(tie, sums, part0, part1, part2, out, grad)
    biases = biases.transpose(1, 0, 2)
    return out, grad, gains, biases, w_in, w_out, w_expand, w_project.transpose(0, 2, 1)


def plain_step(
    tokens, lengths, tie_map, norm_gains, bias_rows, attention_in, attention_out,
    expand_weight, project_weight, cotangent,
):
    slot_rows = tokens.shape[0] // lengths.shape[0]
    me = lax.axis_index("tensor")
    in_local = lax.dynamic_index_in_dim(attention_in, tie_map[0], 0, keepdims=False)
    out_local = lax.dynamic_index_in_dim(attention_out, tie_map[1], 0, keepdims=False)
    expand_local = lax.dynamic_index_in_dim(expand_weight, tie_map[2], 0, keepdims=False)
    project_local = lax.dynamic_index_in_dim(project_weight, tie_map[3], 0, keepdims=False)
    local0 = jnp.concatenate([in_local, out_local.T[None]], 0)
    row_kinds = jnp.array([0, 0, 0, 1, 2, 3] + [2] * (FF // D), dtype=jnp.int32)
    gain_kinds = jnp.array([0, 2], dtype=jnp.int32)
    gain_pick = norm_gains[tie_map[gain_kinds], jnp.arange(2)]
    bias_pick = bias_rows[tie_map[row_kinds], jnp.arange(row_kinds.shape[0])]
    vectors = jnp.concatenate([gain_pick, bias_pick], 0)
    x = lax.dynamic_slice_in_dim(tokens, me * slot_rows, slot_rows, 0)
    cot = lax.dynamic_slice_in_dim(cotangent, me * slot_rows, slot_rows, 0)
    length = lax.dynamic_slice_in_dim(lengths, me, 1, 0)
    rows = lax.all_gather(vectors, ("dp", "tensor"), axis=1, tiled=True).astype(F32)
    rows = jnp.concatenate([rows, jnp.zeros((4, D), F32)], 0)

    def gathered(piece, axis):
        piece = lax.all_gather(piece, "dp", axis=axis, tiled=True)
        return lax.all_gather(piece, "tensor", axis=0)

    g0 = gathered(local0, 1)
    g1 = gathered(expand_local, 0)
    g2 = gathered(project_local.T, 0)
    groups, width = g0.shape[0], g0.shape[-1]
    bqv = rows[3:5].reshape(2, groups, width).transpose(1, 0, 2)
    q, v, kt, p, o, a1t, h1, a2, a2t = run_attention_forward(length, x, g0, rows, bqv)
    out, d1, d2, dh1, gb, gbt, sums = run_feed_forward(length, cot, a2, a2t, h1, g1, g2, rows)
    d0, xg, sums_in, sums_qv = run_attention_backward(
        x, g0, rows, dh1, gb, gbt, q, v, kt, p, o, a1t
    )
    layer_out = lax.all_gather(out, "tensor", axis=0, tiled=True)
    tokens_grad = lax.all_gather(xg, "tensor", axis=0, tiled=True)

    def scattered(piece, axis):
        piece = lax.psum_scatter(piece, "tensor", scatter_dimension=0)
        return lax.psum_scatter(piece, "dp", scatter_dimension=axis, tiled=True).astype(F32)

    part0 = scattered(d0, 1)
    part1 = scattered(d1, 0)
    part2 = scattered(d2, 0)
    qv = sums_qv[:, :2].transpose(1, 0, 2).reshape(2, D)
    sums = jnp.concatenate(
        [sums_in[0:1], sums[1:2], sums_in[1:2], qv, sums[5:12]], 0
    )
    sums = lax.psum_scatter(sums, ("dp", "tensor"), scatter_dimension=1, tiled=True)
    return layer_out, tokens_grad, *placed(tie_map, sums, part0, part1, part2)


def fused_step(
    tokens, lengths, tie_map, norm_gains, bias_rows, attention_in, attention_out,
    expand_weight, project_weight, cotangent,
):
    slots = lengths.shape[0]
    tokens = tokens.reshape(slots, -1, D)
    cotangent = cotangent.reshape(slots, -1, D)
    gq, gw, g1, g2, rows, q, v, kt, p, scale, o, a1t, h1, a2, a2t = run_fused_forward(
        tie_map, lengths, tokens, norm_gains, bias_rows, attention_in, attention_out,
        expand_weight, project_weight,
    )
    layer, fold, work, dh1, gb, gbt, early = run_fused_feed_forward(
        lengths, cotangent, a2, a2t, h1, g1, g2, rows
    )
    grad, out, part0, part1, part2, sums = run_fused_backward(
        tokens, gq, gw, rows, dh1, gb, gbt, q, v, kt, p, scale, o, a1t, layer, fold,
        work, early,
    )
    out, grad, *placed_grads = run_place_gradients(
        tie_map, sums, part0, part1, part2, out, grad,
        (norm_gains, bias_rows, attention_in, attention_out, expand_weight, project_weight),
    )
    return out.reshape(-1, D), grad.reshape(-1, D), *placed_grads


def placed(tie_map, sums, part0, part1, part2):
    source = jnp.arange(NSRC, dtype=jnp.int32)

    def place(piece, which):
        pick = (source == tie_map[which]).reshape((NSRC,) + (1,) * piece.ndim)
        return jnp.where(pick, piece[None], 0.0)

    def place_rows(piece, kinds):
        pick = source[:, None] == tie_map[jnp.array(kinds, dtype=jnp.int32)][None, :]
        return jnp.where(pick[:, :, None], piece[None], 0.0)

    return (
        place_rows(sums[:2], [0, 2]),
        place_rows(sums[2:], [0, 0, 0, 1, 2, 3] + [2] * (FF // D)),
        place(part0[:3], 0),
        place(part0[3].T, 1),
        place(part1, 2),
        place(part2.T, 3),
    )


def solution(mesh):
    fused = mesh.shape["dp"] == Z_DEV * Y_DEV and mesh.shape["tensor"] == X_DEV * C_DEV
    return jax.shard_map(
        fused_step if fused else plain_step,
        mesh=mesh,
        in_specs=(
            P("dp", None),
            P("dp"),
            P(),
            P(None, None, ("dp", "tensor")),
            P(None, None, ("dp", "tensor")),
            P(None, None, "dp", "tensor"),
            P(None, "tensor", "dp"),
            P(None, "dp", "tensor"),
            P(None, "tensor", "dp"),
            P("dp", None),
        ),
        out_specs=(
            P("dp", None),
            P("dp", None),
            P(None, None, ("dp", "tensor")),
            P(None, None, ("dp", "tensor")),
            P(None, None, "dp", "tensor"),
            P(None, "tensor", "dp"),
            P(None, "dp", "tensor"),
            P(None, "tensor", "dp"),
        ),
        check_vma=False,
    )
```

```python
import jax
import jax.numpy as jnp
from jax import lax
from jax.experimental import pallas as pl
from jax.experimental.pallas import tpu as pltpu
from jax.sharding import PartitionSpec as P

D = 768
HEAD_DIM = 64
FF = 3072
NSRC = 4
EPS = 1e-05
MASKED = -1e30
F32 = jnp.float32
BF16 = jnp.bfloat16
VMEM_LIMIT = 60 * 1024 * 1024


def dot_nn(a, b):
    return lax.dot_general(a, b, (((1,), (0,)), ((), ())), preferred_element_type=F32)


def dot_nt(a, b):
    return lax.dot_general(a, b, (((1,), (1,)), ((), ())), preferred_element_type=F32)


def norm_parts(v):
    center = jnp.mean(v, -1, keepdims=True)
    centered = v - center
    r = lax.rsqrt(jnp.mean(centered * centered, -1, keepdims=True) + EPS)
    return centered * r, r


def head_mask(shape, h):
    lane = lax.broadcasted_iota(jnp.int32, shape, 1)
    return (lane >= h * HEAD_DIM) & (lane < (h + 1) * HEAD_DIM)


def blocks(total, size):
    return [slice(i * size, (i + 1) * size) for i in range(total // size)]


def attention_forward(
    len_ref, x_ref, g_ref, rows_ref, bqv_ref,
    q_ref, v_ref, kt_ref, p_ref, o_ref, a1t_ref, h1_ref, a2_ref, a2t_ref,
    a1_ref, k_ref, vt_ref, ot_ref, attn_ref,
):
    t = pl.program_id(0)
    n = x_ref.shape[0]
    width = g_ref.shape[-1]
    heads = width // HEAD_DIM
    step = 256
    length = len_ref[0]

    @pl.when(t == 0)
    def _():
        @pl.loop(0, n // step)
        def _(b):
            rows = pl.ds(pl.multiple_of(b * step, step), step)
            xhat, _ = norm_parts(x_ref[rows, :].astype(F32))
            a1 = xhat * rows_ref[0:1, :] + rows_ref[2:3, :]
            a1_ref[rows, :] = a1.astype(BF16)
            a1t_ref[:, rows] = a1.astype(BF16).T
            attn_ref[rows, :] = x_ref[rows, :].astype(F32) + rows_ref[5:6, :]

    @pl.loop(0, n // step)
    def _(b):
        rows = pl.ds(pl.multiple_of(b * step, step), step)
        a1 = a1_ref[rows, :]
        q = (dot_nn(a1, g_ref[0, 0]) + bqv_ref[0, 0:1, :]).astype(BF16)
        q_ref[0, rows, :] = q * jnp.asarray(HEAD_DIM ** -0.5, BF16)
        k = dot_nn(a1, g_ref[0, 1]).astype(BF16)
        k_ref[rows, :] = k
        kt_ref[0, :, rows] = k.T
        v = (dot_nn(a1, g_ref[0, 2]) + bqv_ref[0, 1:2, :]).astype(BF16)
        v_ref[0, rows, :] = v
        vt_ref[:, rows] = v.T

    for h in range(heads):
        k = k_ref[...]
        k = jnp.where(head_mask(k.shape, h), k, jnp.zeros_like(k))
        for b in range(n // step):
            first, last = b * step, (b + 1) * step
            q = q_ref[0, first:last, :]
            key = lax.broadcasted_iota(jnp.int32, (last, step), 0)
            query = lax.broadcasted_iota(jnp.int32, (step, step), 1) + first
            s = dot_nt(k[:last], q)
            near = jnp.where(
                (key[first:] <= query) & (key[first:] < length), s[first:], MASKED
            )
            if b:
                far = jnp.where(key[:first] < length, s[:first], MASKED)
                top = jnp.maximum(
                    jnp.max(far, 0, keepdims=True), jnp.max(near, 0, keepdims=True)
                )
                e_far = jnp.exp(far - top)
                e_near = jnp.exp(near - top)
                total = jnp.sum(e_far, 0, keepdims=True) + jnp.sum(e_near, 0, keepdims=True)
                scale = 1.0 / total
                p_ref[0, h, :first, first:last] = (e_far * scale).astype(BF16)
            else:
                top = jnp.max(near, 0, keepdims=True)
                e_near = jnp.exp(near - top)
                scale = 1.0 / jnp.sum(e_near, 0, keepdims=True)
            p_ref[0, h, first:last, first:last] = (e_near * scale).astype(BF16)
            ot_ref[h * HEAD_DIM : (h + 1) * HEAD_DIM, first:last] = dot_nn(
                vt_ref[h * HEAD_DIM : (h + 1) * HEAD_DIM, :last],
                p_ref[0, h, :last, first:last],
            ).astype(BF16)

    @pl.loop(0, n // step)
    def _(b):
        rows = pl.ds(pl.multiple_of(b * step, step), step)
        o = ot_ref[:, rows].T
        o_ref[0, rows, :] = o
        attn_ref[rows, :] += dot_nt(o, g_ref[0, 3])

    @pl.when(t == pl.num_programs(0) - 1)
    def _():
        @pl.loop(0, n // step)
        def _(b):
            rows = pl.ds(pl.multiple_of(b * step, step), step)
            h1 = attn_ref[rows, :]
            h1_ref[rows, :] = h1
            xhat, _ = norm_parts(h1)
            a2 = (xhat * rows_ref[1:2, :] + rows_ref[6:7, :]).astype(BF16)
            a2_ref[rows, :] = a2
            a2t_ref[:, rows] = a2.T


SQRT_2_PI = 0.7978845608028654


def feed_forward_both(
    len_ref, c_ref, a2_ref, a2t_ref, h1_ref, w1_ref, w2_ref, rows_ref,
    out_ref, d1_ref, d2_ref, dh1_ref, gb_ref, gbt_ref, sums_ref,
    gf_ref, gft_ref, feed_ref, da2_ref, h_ref, df_ref,
):
    t = pl.program_id(0)
    n = c_ref.shape[0]
    step = 256
    length = len_ref[0]

    @pl.when(t == 0)
    def _():
        sums_ref[...] = jnp.zeros_like(sums_ref)

        @pl.loop(0, n // step)
        def _(b):
            rows = pl.ds(pl.multiple_of(b * step, step), step)
            place = b * step + lax.broadcasted_iota(jnp.int32, (step, 1), 0)
            live = (place < length).astype(F32)
            g = (c_ref[rows, :].astype(F32) * live).astype(BF16)
            gf_ref[rows, :] = g
            gft_ref[:, rows] = g.T
            sums_ref[7:8, :] += jnp.sum(g.astype(F32), 0, keepdims=True)

    bias = rows_ref[pl.ds(8 + t, 1), :]

    @pl.loop(0, n // step)
    def _(b):
        rows = pl.ds(pl.multiple_of(b * step, step), step)
        f = dot_nn(a2_ref[rows, :], w1_ref[0]) + bias
        dh = dot_nn(gf_ref[rows, :], w2_ref[0])
        f2 = f * f
        th = jnp.tanh(f * (SQRT_2_PI + (SQRT_2_PI * 0.044715) * f2))
        half = 0.5 + 0.5 * th
        h = (f * half).astype(BF16)
        slope = half + f * (0.5 - 0.5 * th * th) * (
            SQRT_2_PI + (3 * SQRT_2_PI * 0.044715) * f2
        )
        df = (dh * slope).astype(BF16)
        h_ref[rows, :] = h
        df_ref[rows, :] = df
        sums_ref[pl.ds(8 + t, 1), :] += jnp.sum(df.astype(F32), 0, keepdims=True)
        feed = dot_nt(h, w2_ref[0])
        da2 = dot_nt(df, w1_ref[0])

        @pl.when(t == 0)
        def _():
            feed_ref[rows, :] = feed
            da2_ref[rows, :] = da2

        @pl.when(t > 0)
        def _():
            feed_ref[rows, :] += feed
            da2_ref[rows, :] += da2

    @pl.loop(0, D // step)
    def _(b):
        rows = pl.ds(pl.multiple_of(b * step, step), step)
        d1_ref[0, rows, :] = dot_nn(a2t_ref[rows, :], df_ref[...]).astype(BF16)
        d2_ref[0, rows, :] = dot_nn(gft_ref[rows, :], h_ref[...]).astype(BF16)

    @pl.when(t == pl.num_programs(0) - 1)
    def _():
        @pl.loop(0, n // step)
        def _(b):
            rows = pl.ds(pl.multiple_of(b * step, step), step)
            place = b * step + lax.broadcasted_iota(jnp.int32, (step, 1), 0)
            live = (place < length).astype(F32)
            h1 = h1_ref[rows, :]
            out_ref[rows, :] = (live * (h1 + (feed_ref[rows, :] + rows_ref[7:8, :]))).astype(BF16)
            xhat, r = norm_parts(h1)
            da2 = da2_ref[rows, :]
            sums_ref[1:2, :] += jnp.sum(da2 * xhat, 0, keepdims=True)
            sums_ref[6:7, :] += jnp.sum(da2, 0, keepdims=True)
            dg = da2 * rows_ref[1:2, :]
            dv = r * (
                dg
                - jnp.mean(dg, -1, keepdims=True)
                - xhat * jnp.mean(dg * xhat, -1, keepdims=True)
            )
            dh1 = live * c_ref[rows, :].astype(F32) + dv
            dh1_ref[rows, :] = dh1
            gb = dh1.astype(BF16)
            gb_ref[rows, :] = gb
            gbt_ref[:, rows] = gb.T
            sums_ref[5:6, :] += jnp.sum(gb.astype(F32), 0, keepdims=True)


def attention_backward(
    x_ref, g_ref, rows_ref, dh1_ref, gb_ref, gbt_ref, q_ref, v_ref, kt_ref, p_ref,
    o_ref, a1t_ref,
    d0_ref, xg_ref, sums_ref, bqv_ref,
    do_ref, delta_ref, dqt_ref, dq_ref, dk_ref, dv_ref, da1_ref,
):
    t = pl.program_id(0)
    n = x_ref.shape[0]
    width = g_ref.shape[-1]
    heads = width // HEAD_DIM
    step = 256
    pick = (
        lax.broadcasted_iota(jnp.int32, (16, width), 1) // HEAD_DIM
        == lax.broadcasted_iota(jnp.int32, (16, width), 0)
    ).astype(BF16)

    @pl.loop(0, n // step)
    def _(b):
        rows = pl.ds(pl.multiple_of(b * step, step), step)
        do = dot_nn(gb_ref[rows, :], g_ref[0, 3]).astype(BF16)
        do_ref[rows, :] = do
        prod = do.astype(F32) * o_ref[0, rows, :].astype(F32)
        high = prod.astype(BF16)
        low = (prod - high.astype(F32)).astype(BF16)
        delta_ref[:, rows] = dot_nt(pick, high) + dot_nt(pick, low)

    dqt_ref[...] = jnp.zeros_like(dqt_ref)
    for b in range(n // step):
        first, last = b * step, (b + 1) * step
        do = do_ref[first:, :]
        q = q_ref[0, first:, :]
        v = v_ref[0, first:last, :]
        dk, dv = None, None
        for h in range(heads):
            mine = head_mask((1, width), h)
            zero = jnp.zeros((), BF16)
            p = p_ref[0, h, first:last, first:]
            dp = dot_nt(jnp.where(mine, v, zero), do)
            ds = (p.astype(F32) * (dp - delta_ref[h : h + 1, first:])).astype(BF16)
            part = dot_nn(p, jnp.where(mine, do, zero))
            dv = part if dv is None else dv + part
            part = dot_nn(ds, jnp.where(mine, q, zero))
            dk = part if dk is None else dk + part
            head = slice(h * HEAD_DIM, (h + 1) * HEAD_DIM)
            dqt_ref[head, first:] += dot_nn(kt_ref[0, head, first:last], ds)
        dk_ref[first:last, :] = dk.astype(BF16)
        dv_ref[first:last, :] = dv.astype(BF16)

    @pl.when(t == 0)
    def _():
        da1_ref[...] = jnp.zeros_like(da1_ref)

    bqv_ref[...] = jnp.zeros_like(bqv_ref)

    @pl.loop(0, n // step)
    def _(b):
        rows = pl.ds(pl.multiple_of(b * step, step), step)
        dq = (dqt_ref[:, rows] * HEAD_DIM ** -0.5).astype(BF16).T
        dk = dk_ref[rows, :]
        dv = dv_ref[rows, :]
        dq_ref[rows, :] = dq
        bqv_ref[0, 0:1, :] += jnp.sum(dq.astype(F32), 0, keepdims=True)
        bqv_ref[0, 1:2, :] += jnp.sum(dv.astype(F32), 0, keepdims=True)
        da1_ref[rows, :] += (
            dot_nt(dq, g_ref[0, 0]) + dot_nt(dk, g_ref[0, 1]) + dot_nt(dv, g_ref[0, 2])
        )

    @pl.loop(0, D // step)
    def _(b):
        rows = pl.ds(pl.multiple_of(b * step, step), step)
        a1t = a1t_ref[rows, :]
        d0_ref[0, 0, rows, :] = dot_nn(a1t, dq_ref[...]).astype(BF16)
        d0_ref[0, 1, rows, :] = dot_nn(a1t, dk_ref[...]).astype(BF16)
        d0_ref[0, 2, rows, :] = dot_nn(a1t, dv_ref[...]).astype(BF16)
        d0_ref[0, 3, rows, :] = dot_nn(gbt_ref[rows, :], o_ref[0]).astype(BF16)

    @pl.when(t == pl.num_programs(0) - 1)
    def _():
        sums_ref[...] = jnp.zeros_like(sums_ref)

        @pl.loop(0, n // step)
        def _(b):
            rows = pl.ds(pl.multiple_of(b * step, step), step)
            xhat, r = norm_parts(x_ref[rows, :].astype(F32))
            da1 = da1_ref[rows, :]
            sums_ref[0:1, :] += jnp.sum(da1 * xhat, 0, keepdims=True)
            sums_ref[1:2, :] += jnp.sum(da1, 0, keepdims=True)
            dg = da1 * rows_ref[0:1, :]
            dv = r * (
                dg
                - jnp.mean(dg, -1, keepdims=True)
                - xhat * jnp.mean(dg * xhat, -1, keepdims=True)
            )
            xg_ref[rows, :] = (dh1_ref[rows, :] + dv).astype(BF16)


def whole(*shape):
    return pl.BlockSpec(shape, lambda t: (0,) * len(shape))


def group(*shape):
    return pl.BlockSpec((1,) + shape, lambda t: (t,) + (0,) * len(shape))


def shaped(dtype, *shape):
    return jax.ShapeDtypeStruct(shape, dtype)


SMEM_WHOLE = pl.BlockSpec(memory_space=pltpu.SMEM)


def run_attention_forward(length, x, g0, rows, bqv):
    n = x.shape[0]
    groups, _, _, width = g0.shape
    heads = width // HEAD_DIM
    return pl.pallas_call(
        attention_forward,
        grid=(groups,),
        in_specs=[SMEM_WHOLE, whole(n, D), group(4, D, width), whole(16, D), group(2, width)],
        out_specs=[
            group(n, width), group(n, width), group(width, n), group(heads, n, n),
            group(n, width), whole(D, n), whole(n, D), whole(n, D), whole(D, n),
        ],
        out_shape=[
            shaped(BF16, groups, n, width), shaped(BF16, groups, n, width),
            shaped(BF16, groups, width, n), shaped(BF16, groups, heads, n, n),
            shaped(BF16, groups, n, width), shaped(BF16, D, n), shaped(F32, n, D),
            shaped(BF16, n, D), shaped(BF16, D, n),
        ],
        scratch_shapes=[
            pltpu.VMEM((n, D), BF16), pltpu.VMEM((n, width), BF16),
            pltpu.VMEM((width, n), BF16), pltpu.VMEM((width, n), BF16),
            pltpu.VMEM((n, D), F32),
        ],
        compiler_params=pltpu.CompilerParams(vmem_limit_bytes=VMEM_LIMIT),
        name="attention_forward",
    )(length, x, g0, rows, bqv)


def run_feed_forward(length, cot, a2, a2t, h1, g1, g2, rows):
    n = cot.shape[0]
    groups, _, width = g1.shape
    return pl.pallas_call(
        feed_forward_both,
        grid=(groups,),
        in_specs=[
            SMEM_WHOLE, whole(n, D), whole(n, D), whole(D, n), whole(n, D),
            group(D, width), group(D, width), whole(16, D),
        ],
        out_specs=[
            whole(n, D), group(D, width), group(D, width), whole(n, D), whole(n, D),
            whole(D, n), whole(16, D),
        ],
        out_shape=[
            shaped(BF16, n, D), shaped(BF16, groups, D, width), shaped(BF16, groups, D, width),
            shaped(F32, n, D), shaped(BF16, n, D), shaped(BF16, D, n), shaped(F32, 16, D),
        ],
        scratch_shapes=[
            pltpu.VMEM((n, D), BF16), pltpu.VMEM((D, n), BF16), pltpu.VMEM((n, D), F32),
            pltpu.VMEM((n, D), F32), pltpu.VMEM((n, width), BF16), pltpu.VMEM((n, width), BF16),
        ],
        compiler_params=pltpu.CompilerParams(vmem_limit_bytes=VMEM_LIMIT),
        name="feed_forward_both",
    )(length, cot, a2, a2t, h1, g1, g2, rows)


def run_attention_backward(x, g0, rows, dh1, gb, gbt, q, v, kt, p, o, a1t):
    n = x.shape[0]
    groups, _, _, width = g0.shape
    heads = width // HEAD_DIM
    return pl.pallas_call(
        attention_backward,
        grid=(groups,),
        in_specs=[
            whole(n, D), group(4, D, width), whole(16, D), whole(n, D), whole(n, D),
            whole(D, n), group(n, width), group(n, width), group(width, n),
            group(heads, n, n), group(n, width), whole(D, n),
        ],
        out_specs=[group(4, D, width), whole(n, D), whole(8, D), group(8, width)],
        out_shape=[
            shaped(BF16, groups, 4, D, width), shaped(BF16, n, D), shaped(F32, 8, D),
            shaped(F32, groups, 8, width),
        ],
        scratch_shapes=[
            pltpu.VMEM((n, width), BF16), pltpu.VMEM((16, n), F32), pltpu.VMEM((width, n), F32),
            pltpu.VMEM((n, width), BF16), pltpu.VMEM((n, width), BF16),
            pltpu.VMEM((n, width), BF16), pltpu.VMEM((n, D), F32),
        ],
        compiler_params=pltpu.CompilerParams(vmem_limit_bytes=VMEM_LIMIT),
        name="attention_backward",
    )(x, g0, rows, dh1, gb, gbt, q, v, kt, p, o, a1t)


Z_DEV, Y_DEV, X_DEV, C_DEV = 4, 2, 2, 2


class Place:
    def __init__(self):
        dp, self.t = lax.axis_index("dp"), lax.axis_index("tensor")
        self.dp = dp
        self.z, self.y = dp // 2, dp % 2
        self.x, self.c = self.t // 2, self.t % 2
        self.other_y = 1 - self.y
        self.zs = [
            self.z,
            self.z + 1 - 2 * (self.z % 2),
            self.z + 2 - 4 * (self.z // 2),
            3 - self.z,
        ]
        self.ts = [
            self.t,
            self.t + 1 - 2 * (self.t % 2),
            self.t + 2 - 4 * (self.t // 2),
            3 - self.t,
        ]
        self.to_z = [dict(dp=z * 2 + self.y) for z in self.zs]
        self.to_y = dict(dp=self.z * 2 + self.other_y)
        self.to_x = dict(tensor=self.ts[2])
        self.same_t = self.to_z[1:] + [dict(dp=z * 2 + self.other_y) for z in self.zs]
        self.same_dp = [dict(tensor=t) for t in self.ts[1:]]
        self.to_core = dict(tensor=self.ts[1])

    def group(self, k):
        return lax.select(
            k == 0, self.ts[0],
            lax.select(k == 1, self.ts[1], lax.select(k == 2, self.ts[2], self.ts[3])),
        )

    def greet(self, others=None):
        barrier = pltpu.get_barrier_semaphore()
        others = others or self.to_z[1:] + [self.to_y, self.to_x, self.to_core]
        for device in others:
            pl.semaphore_signal(
                barrier, inc=1, device_id=device, device_id_type=pl.DeviceIdType.MESH
            )
        pl.semaphore_wait(barrier, len(others))


class Pieces:
    def __init__(self, whole, pieces):
        self.whole, self.pieces = whole, pieces

    def start(self):
        for piece in self.pieces:
            piece.start()

    def wait_recv(self):
        self.whole.wait_recv()

    def wait_send(self):
        self.whole.wait_send()


class Links:
    def __init__(self, send_sem, recv_sem):
        self.send_sem, self.recv_sem = send_sem, recv_sem
        self.copies = []

    def add(self, device, src, dst, parts=1, axis=0):
        number = len(self.copies)

        def make(src, dst):
            return pltpu.make_async_remote_copy(
                src_ref=src,
                dst_ref=dst,
                send_sem=self.send_sem.at[number],
                recv_sem=self.recv_sem.at[number],
                device_id=device,
                device_id_type=pl.DeviceIdType.MESH,
            )

        size = src.shape[axis] // parts
        cuts = [(slice(None),) * axis + (pl.ds(i * size, size),) for i in range(parts)]
        copy = Pieces(make(src, dst), [make(src.at[cut], dst.at[cut]) for cut in cuts])
        self.copies.append(copy)
        return copy

    def sent(self, *apart):
        for copy in self.copies:
            if all(copy is not other for other in apart):
                copy.wait_send()


def flat(copies):
    for item in copies:
        if isinstance(item, list):
            yield from flat(item)
        else:
            yield item


def start(*copies):
    for copy in flat(copies):
        copy.start()


def recv(*copies):
    for copy in flat(copies):
        copy.wait_recv()


class Gather:
    def __init__(self, links, place, own, full, order, single=True, last=True):
        every = slice(None)
        y, other = place.y, place.other_y

        def same(device, k, yy, to):
            return links.add(device, full(k, every, yy), full(to, every, yy), Z_DEV)

        def along_z(k, yy, block):
            here, passed = full(k, place.z, yy), full(k, place.zs[2], yy)
            return [
                links.add(place.to_z[1], block, here),
                links.add(place.to_z[2], block, here),
                links.add(place.to_z[1], passed, passed),
            ]

        if order != WHOLE:
            self.z = along_z(0, y, own)
        if order == X_Z_Y:
            self.first = [links.add(place.to_x, own, full(2, place.z, y), 2)]
            self.far = along_z(2, y, full(2, place.z, y))
            blocks = [(0, y), (2, y), (0, other), (2, other)]
        else:
            blocks = [(0, y), (0, other), (2, y), (2, other)]
        if order == Y_Z_X:
            self.first = [links.add(place.to_y, own, full(0, place.z, y), 2)]
            self.far = along_z(0, other, full(0, place.z, other))
        if order == Z_Y_X and single:
            self.first = [same(place.to_y, 0, y, 0)]
        if order == Z_Y_X and not single:
            self.first = [links.add(place.to_y, own, full(0, place.z, y))]
            for k in range(1, 4):
                block = full(0, place.zs[k], y)
                self.first.append(links.add(place.to_y, block, block))
            return
        self.second = [
            same(place.to_y, k, yy, k) if order == X_Z_Y else same(place.to_x, k, yy, 2)
            for k, yy in blocks[: 2 if last else 1]
        ]
        if not last:
            blocks = [block for block in blocks if block[0] == 0]
        self.core = [same(place.to_core, k, yy, k + 1) for k, yy in blocks]


Z_Y_X, Y_Z_X, X_Z_Y, WHOLE = range(4)


def fused_forward(
    tie_ref, len_ref, tokens_ref, gains_ref, bias_ref, in_ref, out_ref, expand_ref,
    project_ref,
    gq_ref, gw_ref, flat1_ref, flat2_ref, rows_ref,
    q_ref, v_ref, kt_ref, p_ref, scale_ref, o_ref, a1t_out, h1_out, a2_out, a2t_out,
    own0_ref, own1_ref, own2_ref, square_ref, vec_ref,
    all0_ref, w1_ref, w2_ref, vecs_ref, bqv_ref, x_ref, a1_ref, k_ref, qa_ref, vt_ref, ot_ref, a1t_ref, h1_ref, a2_ref, a2t_ref,
    send_sem, recv_sem, local_sem, flush_sem, row_sem,
):
    t, h = pl.program_id(0), pl.program_id(1)
    n, _ = x_ref.shape
    width = q_ref.shape[-1]
    heads = width // HEAD_DIM
    step = 256
    place = Place()
    length = len_ref[place.t]
    links = Links(send_sem, recv_sem)
    z, y, x, c = place.z, place.y, place.x, place.c
    mine_there = vecs_ref.at[z, y, x, c]
    column = vecs_ref.at[:, :, x, c]
    vec_one = [links.add(device, vec_ref, mine_there) for device in place.same_t]
    vec_two = [links.add(device, column, column) for device in place.same_dp]
    half = own0_ref.shape[0] // 2
    halves = []
    for i in range(2):
        rows = pl.ds(i * half, half)
        halves.append(Gather(
            links, place, own0_ref.at[rows],
            lambda k, z, y, rows=rows: all0_ref.at[k, z, y, rows], Z_Y_X, single=False,
        ))
    seg0 = Gather(links, place, own0_ref, lambda k, z, y: all0_ref.at[k, z, y], WHOLE)
    seg1 = Gather(
        links, place, own1_ref, lambda k, z, y: w1_ref.at[k, z, y], Y_Z_X, last=False
    )
    seg2 = Gather(
        links, place, own2_ref, lambda k, z, y: w2_ref.at[k, z, y], X_Z_Y, last=False
    )
    flush = [
        [
            pltpu.make_async_copy(ref.at[k], flat.at[k], flush_sem.at[i, k])
            for k in range(3)
        ]
        for i, (ref, flat) in enumerate([(w1_ref, flat1_ref), (w2_ref, flat2_ref)])
    ]
    put_a1t = pltpu.make_async_copy(a1t_ref, a1t_out, local_sem.at[0])
    put_a2t = pltpu.make_async_copy(a2t_ref, a2t_out, local_sem.at[1])
    puts = []
    for i in range(n // step):
        rows = pl.ds(i * step, step)
        puts.append([
            pltpu.make_async_copy(h1_ref.at[rows], h1_out.at[rows], row_sem.at[0, i]),
            pltpu.make_async_copy(a2_ref.at[rows], a2_out.at[rows], row_sem.at[1, i]),
        ])
    fetch = pltpu.make_async_copy(tokens_ref.at[place.t], x_ref, local_sem.at[2])

    def relay_z(copies):
        recv(copies[1])
        start(copies[2])

    def pass_own(seg):
        recv(seg.z[0], seg.z[2])
        start(seg.second[0], seg.core[0])

    def pass_second(seg):
        recv(seg.second)
        if seg is seg2:
            start(seg.core[1])

    def pass_first(seg):
        recv(seg.first)
        start(seg.far[1], seg.far[0])

    def pass_far(seg):
        recv(seg.far[0], seg.far[2])
        start(seg.core[1:] if seg is seg1 else [])

    def pass_core(seg, i):
        recv(seg.second[i])
        start(seg.core[2 + i])

    plan = [
        (0, 0, lambda: (pass_first(seg1), relay_z(seg2.z), pass_first(seg2))),
        (0, 3, lambda: (relay_z(seg1.z), pass_core(seg0, 0))),
        (1, 0, lambda: recv(seg0.core[:2])),
        (1, 1, lambda: relay_z(seg1.far)),
        (1, 3, lambda: pass_core(seg0, 1)),
        (1, 4, lambda: pass_own(seg2)),
        (2, 1, lambda: relay_z(seg2.far)),
        (2, 3, lambda: pass_own(seg1)),
        (3, 0, lambda: (recv(seg0.core[2:]), pass_far(seg1), flush[0][0].start())),
        (3, 2, lambda: (pass_second(seg2), flush[1][0].start())),
        (3, 3, lambda: (pass_far(seg2), flush[1][2].start())),
    ]

    def serve(points):
        for step, where, act in plan:
            if where in points:
                now = (t == step) & (h == max(where - 2, 0))
                pl.when(now)(lambda act=act: (act(), None)[1])

    @pl.when((t == 0) & (h == 0))
    def _():
        s0, s1, s2, s3 = tie_ref[0], tie_ref[1], tie_ref[2], tie_ref[3]
        fetch.start()
        square_ref[...] = jnp.zeros_like(square_ref)
        gain = gains_ref.shape[-1]
        square_ref[0:1, :gain] = gains_ref[s0].astype(F32)[0:1]
        square_ref[1:2, :gain] = gains_ref[s2].astype(F32)[1:2]
        kinds = [s0, s0, s0, s1, s2, s3, s2, s2, s2, s2]
        for i, source in enumerate(kinds):
            wide = bias_ref[i].astype(F32)
            here = lax.broadcasted_iota(jnp.int32, wide.shape, 0) == source
            square_ref[2 + i : 3 + i, :gain] = jnp.sum(
                jnp.where(here, wide, 0.0), 0, keepdims=True
            )
        vec_ref[...] = square_ref[...].T[:gain]
        for j in range(3):
            own0_ref[:, j * width : (j + 1) * width] = in_ref[s0, j]
        own0_ref[:, 3 * width :] = out_ref[s1].T
        place.greet(place.same_t + place.same_dp)
        start(vec_one)
        for part in halves:
            start(part.z[1], part.z[0], part.first[0])
        vecs_ref[z, y, x, c] = vec_ref[...]
        ones = lax.broadcasted_iota(jnp.int32, (vt_ref.shape[1] - HEAD_DIM, n), 0) == 0
        for h in range(heads):
            vt_ref[h, HEAD_DIM:, :] = ones.astype(BF16)
        all0_ref[0, z, y] = own0_ref[...]
        own1_ref[...] = expand_ref[s2]
        own2_ref[...] = project_ref[s3]
        w1_ref[0, z, y] = own1_ref[...]
        w2_ref[0, z, y] = own2_ref[...]
        recv(vec_one)
        start(vec_two)
        for part in halves:
            relay_z(part.z)
            start(part.first[2])
        for part in halves:
            recv(part.z[0])
            start(part.first[1])
        start(seg2.z[1])
        recv(vec_two)
        start(seg2.first)
        vecs = vecs_ref[...].reshape(D, vecs_ref.shape[-1]).T[:16]
        rows_ref[...] = vecs
        for part in halves:
            recv(part.z[2])
            start(part.first[3])
        start(seg1.first, seg0.second[0], seg0.core[0])
        for k in range(4):
            part = slice(k * width, (k + 1) * width)
            bqv_ref[k, 0:1, :width] = vecs[3:4, part]
            bqv_ref[k, 0:1, width : 2 * width] = jnp.zeros((1, width), F32)
            bqv_ref[k, 0:1, 2 * width :] = vecs[4:5, part]
        fetch.wait()

        @pl.loop(0, n // step)
        def _(b):
            rows = pl.ds(pl.multiple_of(b * step, step), step)
            wide = x_ref[rows, :].astype(F32)
            xhat, _ = norm_parts(wide)
            a1 = (xhat * rows_ref[0:1, :] + rows_ref[2:3, :]).astype(BF16)
            a1_ref[rows, :] = a1
            a1t_ref[:, rows] = a1.T
            h1_ref[rows, :] = wide + rows_ref[5:6, :]

        put_a1t.start()
        start(seg2.z[0], seg1.z[1], seg1.z[0])
        recv(halves[0].first, halves[1].first)
        start(seg0.second[1], seg0.core[1])

    serve([0])

    @pl.when(h == 0)
    def _():
        here = all0_ref[t].reshape(D, 4 * width)
        gq = here[:, : 3 * width]
        gq_ref[0] = gq
        gw_ref[0] = here[:, 3 * width :]
        mine = place.group(t)
        qkv = dot_nn(a1_ref[...], gq) + bqv_ref[mine, 0:1, :]
        q = qkv[:, :width].astype(BF16) * jnp.asarray(HEAD_DIM ** -0.5, BF16)
        k = qkv[:, width : 2 * width].astype(BF16)
        v = qkv[:, 2 * width :].astype(BF16)
        q_ref[0] = q
        kt_ref[0] = k.T
        v_ref[0] = v
        vt = v.T
        for h in range(heads):
            vt_ref[h, :HEAD_DIM, :] = vt[h * HEAD_DIM : (h + 1) * HEAD_DIM]
        spare = k_ref.shape[1] - width
        dead = lax.broadcasted_iota(jnp.int32, (n, spare), 0) >= length
        first_column = lax.broadcasted_iota(jnp.int32, (n, spare), 1) == 0
        k_ref[:, :width] = k
        k_ref[:, width:] = jnp.where(first_column & dead, MASKED, 0.0).astype(BF16)
        qa_ref[:, :width] = q
        qa_ref[:, width:] = jnp.where(first_column, 1.0, 0.0).astype(BF16)
        scale_ref[0, heads:, :] = jnp.zeros((scale_ref.shape[1] - heads, n), F32)

    serve([1])

    lane = lax.broadcasted_iota(jnp.int32, (1, qa_ref.shape[1]), 1)
    keep = ((lane >= h * HEAD_DIM) & (lane < (h + 1) * HEAD_DIM)) | (lane >= width)
    key = lax.broadcasted_iota(jnp.int32, (step, step), 0)
    query = lax.broadcasted_iota(jnp.int32, (step, step), 1)
    head = pl.ds(pl.multiple_of(h * HEAD_DIM, HEAD_DIM), HEAD_DIM)

    def scores(b):
        first, last = b * step, (b + 1) * step
        q = jnp.where(keep, qa_ref[first:last, :], jnp.zeros((), BF16))
        return dot_nt(k_ref[:last, :], q)

    def attend(b, s):
        first, last = b * step, (b + 1) * step
        near = jnp.where(key <= query, s[first:], MASKED)
        top = jnp.max(near, 0, keepdims=True)
        if b:
            far = s[:first]
            top = jnp.maximum(top, jnp.max(far, 0, keepdims=True))
        e_near = jnp.exp((near - top).astype(BF16))
        p_ref[0, 0, b, first:last, :] = e_near
        o = dot_nn(vt_ref[h, :, first:last], e_near)
        if b:
            e_far = jnp.exp((far - top).astype(BF16))
            p_ref[0, 0, b, :first, :] = e_far
            o += dot_nn(vt_ref[h, :, :first], e_far)
        scale = 1.0 / o[HEAD_DIM : HEAD_DIM + 1]
        scale_ref[0, pl.ds(h, 1), first:last] = scale
        ot_ref[head, first:last] = (o[:HEAD_DIM] * scale).astype(BF16)

    s = scores(0)
    for b in range(n // step):
        ahead = scores(b + 1) if b + 1 < n // step else None
        attend(b, s)
        s = ahead

    serve([2, 3, 4])

    @pl.when(h == heads - 1)
    def _():
        o = ot_ref[...].T
        o_ref[0] = o
        h1_ref[...] += dot_nt(o, gw_ref[0])

    @pl.when((t == 3) & (h == heads - 1))
    def _():
        for i, rows in enumerate(blocks(n, step)):
            xhat, _ = norm_parts(h1_ref[rows, :])
            a2 = (xhat * rows_ref[1:2, :] + rows_ref[6:7, :]).astype(BF16)
            a2_ref[rows, :] = a2
            a2t_ref[:, rows] = a2.T
            for put in puts[i]:
                put.start()
        put_a2t.start()
        recv(seg2.core)
        flush[1][1].start()
        recv(seg1.core)
        flush[0][1].start()
        pass_second(seg1)
        flush[0][2].start()
        links.sent()
        for copies in flush + puts + [[put_a1t, put_a2t]]:
            for copy in copies:
                copy.wait()


N_GATHER = 10 + 14 + 6 + 10 + 10
VMEM_WHOLE = pl.BlockSpec(memory_space=pltpu.VMEM)
ANY_WHOLE = pl.BlockSpec(memory_space=pl.ANY)


def run_fused_forward(tie, lengths, tokens, gains, biases, w_in, w_out, w_expand, w_project):
    groups, n, _ = tokens.shape
    depth, width = w_in.shape[-2:]
    heads = width // HEAD_DIM
    hidden = w_expand.shape[-1]
    w_project = w_project.transpose(0, 2, 1)
    biases = biases.transpose(1, 0, 2)
    own = gains.shape[-1]

    def group(*shape):
        return pl.BlockSpec((1,) + shape, lambda t, h: (t,) + (0,) * len(shape))

    per_head = pl.BlockSpec((1, 1, n // 256, n, 256), lambda t, h: (t, h, 0, 0, 0))
    return pl.pallas_call(
        fused_forward,
        grid=(groups, heads),
        in_specs=[SMEM_WHOLE, SMEM_WHOLE, ANY_WHOLE] + [VMEM_WHOLE] * 6,
        out_specs=[
            group(D, 3 * width), group(D, width), ANY_WHOLE, ANY_WHOLE, VMEM_WHOLE,
            group(n, width), group(n, width), group(width, n), per_head,
            group(8, n), group(n, width), ANY_WHOLE, ANY_WHOLE, ANY_WHOLE, ANY_WHOLE,
        ],
        out_shape=[
            shaped(BF16, groups, D, 3 * width), shaped(BF16, groups, D, width),
            shaped(BF16, groups, Z_DEV, Y_DEV, depth, hidden),
            shaped(BF16, groups, Z_DEV, Y_DEV, depth, hidden),
            shaped(F32, 16, D),
            shaped(BF16, groups, n, width), shaped(BF16, groups, n, width),
            shaped(BF16, groups, width, n), shaped(BF16, groups, heads, n // 256, n, 256),
            shaped(F32, groups, 8, n), shaped(BF16, groups, n, width), shaped(BF16, D, n), shaped(F32, n, D),
            shaped(BF16, n, D), shaped(BF16, D, n),
        ],
        scratch_shapes=[
            pltpu.VMEM((depth, 4 * width), BF16),
            pltpu.VMEM((depth, hidden), BF16), pltpu.VMEM((depth, hidden), BF16),
            pltpu.VMEM((128, 128), F32), pltpu.VMEM((own, 128), F32),
            pltpu.VMEM((groups, Z_DEV, Y_DEV, depth, 4 * width), BF16),
            pltpu.VMEM((groups, Z_DEV, Y_DEV, depth, hidden), BF16),
            pltpu.VMEM((groups, Z_DEV, Y_DEV, depth, hidden), BF16),
            pltpu.VMEM((Z_DEV, Y_DEV, X_DEV, C_DEV, own, 128), F32),
            pltpu.VMEM((groups, 8, 3 * width), F32),
            pltpu.VMEM((n, D), BF16), pltpu.VMEM((n, D), BF16), pltpu.VMEM((n, 256), BF16),
            pltpu.VMEM((n, 256), BF16), pltpu.VMEM((heads, HEAD_DIM + 16, n), BF16),
            pltpu.VMEM((width, n), BF16),
            pltpu.VMEM((D, n), BF16), pltpu.VMEM((n, D), F32), pltpu.VMEM((n, D), BF16),
            pltpu.VMEM((D, n), BF16),
            pltpu.SemaphoreType.DMA((N_GATHER,)), pltpu.SemaphoreType.DMA((N_GATHER,)),
            pltpu.SemaphoreType.DMA((3,)), pltpu.SemaphoreType.DMA((2, 4)),
            pltpu.SemaphoreType.DMA((2, n // 256)),
        ],
        compiler_params=pltpu.CompilerParams(
            vmem_limit_bytes=VMEM_LIMIT, collective_id=0, has_side_effects=True
        ),
        name="fused_forward",
    )(tie, lengths, tokens, gains, biases, w_in, w_out, w_expand, w_project)


class Result:
    def __init__(self, links, place, own_ref, passing_ref, out_ref, step, sem, count):
        self.x, self.core, self.far, self.keep, self.keep_far = [], [], [], [], []
        for i in range(count):
            rows = pl.ds(i * step, step)
            mine, theirs = out_ref.at[place.t, rows], out_ref.at[place.ts[2], rows]
            own, passing = own_ref.at[rows], passing_ref.at[rows]
            self.x.append(links.add(place.to_x, own, passing))
            self.core.append(links.add(place.to_core, own, mine))
            self.far.append(links.add(place.to_core, passing, theirs))
            self.keep.append(pltpu.make_async_copy(own, mine, sem.at[0, i]))
            self.keep_far.append(pltpu.make_async_copy(passing, theirs, sem.at[1, i]))

    def send(self, i):
        start(self.x[i], self.core[i], self.keep[i])

    def pass_on(self, i):
        recv(self.x[i])
        start(self.far[i], self.keep_far[i])

    def finish(self):
        recv(self.core, self.far)
        for copy in self.keep + self.keep_far:
            copy.wait()


def low(value):
    return jnp.asarray(value, BF16)


def pair_order(i):
    return i + 1 - 2 * (i % 2)


def fused_feed_forward(
    len_ref, cot_ref, a2_ref, a2t_in, h1_in, far1_ref, far2_ref, rows_ref,
    out_out, fold_ref, work_out, dh1_out, gb_out, gbt_out, sums_ref,
    gf_ref, gft_ref, feed_ref, da2_ref, h_ref, df_ref, weights_ref, missing_ref, third_ref,
    stage_ref, land_ref, near_ref, cross_ref, a2t_ref, h1_ref, out_ref, work_ref,
    send_sem, recv_sem, local_sem, row_sem,
):
    t = pl.program_id(0)
    n = gf_ref.shape[0]
    step = 256
    depth = stage_ref.shape[-2]
    place = Place()
    length = len_ref[place.t]
    links = Links(send_sem, recv_sem)
    y, other = place.y, place.other_y
    last = [
        links.add(place.to_x, far1_ref.at[0, :, other], missing_ref.at[0, 0]),
        links.add(place.to_y, far2_ref.at[2, :, y], missing_ref.at[1, 0]),
    ]
    last_core = [
        links.add(place.to_core, missing_ref.at[i, 0], missing_ref.at[i, 1]) for i in range(2)
    ]
    third = [
        links.add(place.to_core, far_ref.at[2, :, y], third_ref.at[i])
        for i, far_ref in enumerate([far1_ref, far2_ref])
    ]
    core = [
        [links.add(place.to_core, stage_ref.at[i], land_ref.at[s, i]) for i in range(2)]
        for s in range(2)
    ]
    cross = [
        links.add(place.to_y, near_ref.at[i, :, other], cross_ref.at[i]) for i in range(2)
    ]
    fetch = pltpu.make_async_copy(cot_ref.at[place.t], gf_ref, local_sem.at[0])
    gb_ref, gbt_ref, dh1_ref = gf_ref, gft_ref, da2_ref
    late = [
        pltpu.make_async_copy(a2t_in, a2t_ref, local_sem.at[5]),
        pltpu.make_async_copy(h1_in, h1_ref, local_sem.at[6]),
    ]
    puts = []
    for i in range(n // step):
        rows = pl.ds(i * step, step)
        puts.append([
            pltpu.make_async_copy(ref.at[rows], out.at[rows], row_sem.at[j, i])
            for j, (ref, out) in enumerate(
                [(out_ref, out_out), (dh1_ref, dh1_out), (gb_ref, gb_out)]
            )
        ])
    put_gbt = pltpu.make_async_copy(gbt_ref, gbt_out, local_sem.at[7])
    put_work = pltpu.make_async_copy(work_ref, work_out, local_sem.at[8])
    k = pair_order(t)
    mine = place.group(k)

    def load(step, whole, slot):
        for i, far_ref in enumerate([far1_ref, far2_ref]):
            group = far_ref.at[pair_order(step)]
            to = weights_ref.at[slot, i]
            if not whole:
                group, to = group.at[:, y], to.at[:, y]
            yield pltpu.make_async_copy(group, to, local_sem.at[1 + 2 * slot + i])

    def live_rows(b):
        at = b * step + lax.broadcasted_iota(jnp.int32, (step, 1), 0)
        return (at < length).astype(F32)

    @pl.when(t == 0)
    def _():
        fetch.start()
        for copy in load(0, True, 0):
            copy.start()
        for copy in late:
            copy.start()
        place.greet()
        start(last, third)
        sums_ref[...] = jnp.zeros_like(sums_ref)
        feed_ref[...] = jnp.zeros_like(feed_ref)
        da2_ref[...] = jnp.zeros_like(da2_ref)
        fetch.wait()

        @pl.loop(0, n // step)
        def _(b):
            rows = pl.ds(pl.multiple_of(b * step, step), step)
            g = (gf_ref[rows, :].astype(F32) * live_rows(b)).astype(BF16)
            gf_ref[rows, :] = g
            gft_ref[:, rows] = g.T
            sums_ref[7:8, :] += jnp.sum(g.astype(F32), 0, keepdims=True)

    for i in range(4):
        @pl.when(t == i)
        def _():
            if i == 2:
                recv(last_core, third)
            else:
                for copy in load(i, i < 2, i % 2):
                    copy.wait()
            if i in (0, 2):
                for copy in load(i + 1, i + 1 < 2, (i + 1) % 2):
                    copy.start()
            for j in range(2):
                if i == 2:
                    weights_ref[0, j, :, y] = third_ref[j]
                if i >= 2:
                    weights_ref[i % 2, j, :, other] = missing_ref[j, 3 - i]

    bias = rows_ref[pl.ds(8 + mine, 1), :]
    w1 = weights_ref[t % 2, 0].reshape(D, -1)
    w2 = weights_ref[t % 2, 1].reshape(D, -1)
    column = jnp.zeros((1, w1.shape[1]), F32)
    for rows in blocks(n, step):
        f = (dot_nn(a2_ref[rows, :], w1) + bias).astype(BF16)
        dh = dot_nn(gf_ref[rows, :], w2)
        f2 = f * f
        th = jnp.tanh(f * (low(SQRT_2_PI) + low(SQRT_2_PI * 0.044715) * f2))
        half = low(0.5) + low(0.5) * th
        h = f * half
        slope = half + f * (low(0.5) - low(0.5) * th * th) * (
            low(SQRT_2_PI) + low(3 * SQRT_2_PI * 0.044715) * f2
        )
        df = (dh * slope.astype(F32)).astype(BF16)
        h_ref[rows, :] = h
        df_ref[rows, :] = df
        column += jnp.sum(df.astype(F32), 0, keepdims=True)
        feed_ref[rows, :] += dot_nt(h, w2)
        da2_ref[rows, :] += dot_nt(df, w1)
    sums_ref[pl.ds(8 + mine, 1), :] = column

    @pl.when(t == 1)
    def _():
        recv(last)
        start(last_core)

    @pl.when(t == 0)
    def _():
        late[0].wait()

    def weight_grad(left_ref, right_ref):
        value = dot_nn(left_ref[...], right_ref[...])
        return value.reshape(Z_DEV, Y_DEV, depth, value.shape[-1]).astype(BF16)

    grad1 = weight_grad(a2t_ref, df_ref)
    grad2 = weight_grad(gft_ref, h_ref)

    def put(ref):
        ref[0] = grad1
        ref[1] = grad2

    def reduced(ref):
        return lambda i, s, z: (
            ref[i, z].astype(F32) + land_ref[s, i, z].astype(F32)
        ).astype(BF16)

    @pl.when(t == 0)
    def _():
        put(stage_ref)
        start(core[0])

    @pl.when(t == 1)
    def _():
        put(near_ref)
        recv(core[0])

        @pl.loop(0, Z_DEV)
        def _(z):
            for i in range(2):
                near_ref[i, z] = reduced(near_ref)(i, 0, z)

        start(cross)

    @pl.when(t == 2)
    def _():
        for copy in core[0]:
            copy.wait_send()
        put(stage_ref)
        start(core[1])

    @pl.when(t == 3)
    def _():
        put(work_ref)
        late[1].wait()
        for i, rows in enumerate(blocks(n, step)):
            live = live_rows(i)
            h1 = h1_ref[rows, :]
            out_ref[rows, :] = (live * (h1 + (feed_ref[rows, :] + rows_ref[7:8, :]))).astype(BF16)
            xhat, r = norm_parts(h1)
            da2 = da2_ref[rows, :]
            sums_ref[1:2, :] += jnp.sum(da2 * xhat, 0, keepdims=True)
            sums_ref[6:7, :] += jnp.sum(da2, 0, keepdims=True)
            dg = da2 * rows_ref[1:2, :]
            dv = r * (
                dg
                - jnp.mean(dg, -1, keepdims=True)
                - xhat * jnp.mean(dg * xhat, -1, keepdims=True)
            )
            dh1 = gf_ref[rows, :].astype(F32) + dv
            dh1_ref[rows, :] = dh1
            gb = dh1.astype(BF16)
            gb_ref[rows, :] = gb
            gbt_ref[:, rows] = gb.T
            sums_ref[5:6, :] += jnp.sum(gb.astype(F32), 0, keepdims=True)
            for copy in puts[i]:
                copy.start()
        put_gbt.start()
        recv(core[1])

        @pl.loop(0, Z_DEV)
        def _(z):
            for i in range(2):
                work_ref[i, z] = reduced(work_ref)(i, 1, z)

        put_work.start()
        recv(cross)

        @pl.loop(0, Z_DEV)
        def _(z):
            for i in range(2):
                fold_ref[i, z] = (
                    near_ref[i, z, y].astype(F32) + cross_ref[i, z].astype(F32)
                ).astype(BF16)

        links.sent(*core[0])
        for copies in puts + [[put_gbt, put_work]]:
            for copy in copies:
                copy.wait()


def run_fused_feed_forward(lengths, cot, a2, a2t, h1, g1, g2, rows):
    n = cot.shape[1]
    groups, _, _, depth, hidden = g1.shape
    both = (2, Z_DEV, Y_DEV, depth, hidden)
    fold = (2, Z_DEV, depth, hidden)
    return pl.pallas_call(
        fused_feed_forward,
        grid=(groups,),
        in_specs=[SMEM_WHOLE, ANY_WHOLE, VMEM_WHOLE] + [ANY_WHOLE] * 4 + [VMEM_WHOLE],
        out_specs=[ANY_WHOLE, VMEM_WHOLE] + [ANY_WHOLE] * 4 + [VMEM_WHOLE],
        out_shape=[
            shaped(BF16, n, D), shaped(BF16, *fold), shaped(BF16, *both), shaped(F32, n, D),
            shaped(BF16, n, D), shaped(BF16, D, n), shaped(F32, 16, D),
        ],
        scratch_shapes=[
            pltpu.VMEM((n, D), BF16), pltpu.VMEM((D, n), BF16), pltpu.VMEM((n, D), F32),
            pltpu.VMEM((n, D), F32), pltpu.VMEM((n, hidden), BF16), pltpu.VMEM((n, hidden), BF16),
            pltpu.VMEM((2,) + both, BF16),
            pltpu.VMEM((2,) + fold, BF16), pltpu.VMEM(fold, BF16), pltpu.VMEM(both, BF16),
            pltpu.VMEM((2,) + both, BF16),
            pltpu.VMEM(both, BF16), pltpu.VMEM(fold, BF16),
            pltpu.VMEM((D, n), BF16), pltpu.VMEM((n, D), F32), pltpu.VMEM((n, D), BF16),
            pltpu.VMEM(both, BF16),
            pltpu.SemaphoreType.DMA((12,)), pltpu.SemaphoreType.DMA((12,)),
            pltpu.SemaphoreType.DMA((9,)), pltpu.SemaphoreType.DMA((3, n // 256)),
        ],
        compiler_params=pltpu.CompilerParams(
            vmem_limit_bytes=VMEM_LIMIT, collective_id=1, has_side_effects=True
        ),
        name="fused_feed_forward",
    )(lengths, cot, a2, a2t, h1, g1, g2, rows)
class Reduce:
    def __init__(
        self, links, place, work, acc, cross_ref, far_ref, mid_ref, last_ref, side_ref,
        slots=(0, 1),
    ):
        self.place, self.work, self.acc = place, work, acc
        self.cross_ref, self.far_ref, self.mid_ref = cross_ref, far_ref, mid_ref
        self.last_ref, self.side_ref = last_ref, side_ref
        self.two = len(slots) == 2
        zs = place.zs
        self.y = {
            s: [
                links.add(
                    place.to_y, work(s, zs[j], place.other_y),
                    cross_ref.at[s if self.two else 0, zs[j]],
                )
                for j in (1, 3, 2, 0)
            ]
            for s in slots
        }
        self.z = [
            [
                links.add(place.to_z[1], acc(s, zs[1]), far_ref.at[s, 0]),
                links.add(place.to_z[1], acc(s, zs[3]), far_ref.at[s, 1]),
                links.add(place.to_z[2], mid_ref.at[s, 1], far_ref.at[s, 2]),
            ]
            for s in range(2)
        ]
        self.x = links.add(place.to_x, last_ref, side_ref)

    def fold_y(self, s, half):
        for i, j in [(0, 1), (1, 3), (2, 2), (3, 0)][2 * half : 2 * half + 2]:
            z = self.place.zs[j]
            recv(self.y[s][i])
            value = self.work(s, z, self.place.y)[...].astype(F32)
            cross = self.cross_ref[s if self.two else 0, z].astype(F32)
            self.acc(s, z)[...] = (value + cross).astype(BF16)
            if i < 2:
                start(self.z[s][i])

    def fold_z(self, s):
        recv(self.z[s][:2])
        for i in (1, 0):
            value = self.acc(s, self.place.zs[2 * i])[...].astype(F32)
            self.mid_ref[s, i] = (value + self.far_ref[s, i].astype(F32)).astype(BF16)
            if i:
                start(self.z[s][2])

    def own(self, s):
        recv(self.z[s][2])
        return self.mid_ref[s, 0].astype(F32) + self.far_ref[s, 2].astype(F32)

    def send_x(self):
        self.last_ref[...] = self.own(1).astype(BF16)
        start(self.x)

    def total(self):
        value = self.own(0)
        recv(self.x)
        return value + self.side_ref[...].astype(F32)


def fused_backward(
    tokens_ref, gq_in, gw_in, rows_ref, dh1_ref, gb_ref, gbt_in, q_in, v_in, kt_in,
    p_ref, scale_in, o_in, a1t_in, layer_in, fold_in, work_in, early_ref,
    out_ref, layerout_ref, part0_ref, part1_ref, part2_ref, total_ref,
    gq_ref, gw_ref, q_ref, v_ref, kt_ref, scale_ref, o_ref,
    a1t_ref, gbt_ref, layer_ref, fold_ref, work_ref, do_ref, delta_ref, dkv_ref, dqkv_ref, hold_ref, da1_ref, own_ref, passing_ref, passlayer_ref, bqv_ref,
    folded_ref, cross1_ref, far1_ref, mid1_ref, last1_ref, side1_ref,
    cross2_ref, far2_ref, mid2_ref, last2_ref, side2_ref,
    stage0_ref, land0_ref, work0_ref, cross0_ref, far0_ref, mid0_ref, last0_ref, side0_ref,
    sums_ref, sumland_ref,
    send_sem, recv_sem, local_sem, result_sem, group_sem,
):
    t = pl.program_id(0)
    n = own_ref.shape[0]
    width = gw_ref.shape[-1]
    depth = part0_ref.shape[0]
    heads = width // HEAD_DIM
    step = n // 4
    place = Place()
    y = place.y
    links = Links(send_sem, recv_sem)
    k, i = group_and_block(t)
    mine = place.group(k)
    now = k % 2
    out = Result(links, place, own_ref, passing_ref, out_ref, step, result_sem.at[0], 4)
    layer = Result(links, place, layer_ref, passlayer_ref, layerout_ref, step, result_sem.at[1], 4)
    fetch = pltpu.make_async_copy(tokens_ref.at[place.t], own_ref, local_sem.at[0])
    fetch_layer, fetch_work, fetch_fold, fetch_gbt, fetch_a1t = [
        pltpu.make_async_copy(there, here, local_sem.at[1 + j])
        for j, (there, here) in enumerate([
            (layer_in, layer_ref), (work_in, work_ref), (fold_in, fold_ref),
            (gbt_in, gbt_ref), (a1t_in, a1t_ref),
        ])
    ]
    def operands(group):
        slot = group % 2
        pairs = [
            (gw_in, gw_ref), (scale_in, scale_ref), (o_in, o_ref), (v_in, v_ref),
            (q_in, q_ref), (kt_in, kt_ref), (gq_in, gq_ref),
        ]
        return [
            pltpu.make_async_copy(there.at[group], here.at[slot], group_sem.at[slot, j])
            for j, (there, here) in enumerate(pairs)
        ]

    core0 = [links.add(place.to_core, stage0_ref, land0_ref.at[i]) for i in range(2)]
    def half_done(i, *landing):
        return Reduce(
            links, place, lambda s, z, y: work_ref.at[i, z, y],
            lambda s, z: folded_ref.at[i, z] if s else fold_ref.at[i, z],
            *landing, slots=(1,),
        )

    seg1 = half_done(0, cross1_ref, far1_ref, mid1_ref, last1_ref, side1_ref)
    seg2 = half_done(1, cross2_ref, far2_ref, mid2_ref, last2_ref, side2_ref)
    seg0 = Reduce(
        links, place, lambda s, z, y: work0_ref.at[s, z, y],
        lambda s, z: work0_ref.at[s, z, y],
        cross0_ref, far0_ref, mid0_ref, last0_ref, side0_ref,
    )
    sum_core, sum_y, *sum_z, sum_x = [
        links.add(to, sums_ref.at[i], sumland_ref.at[j])
        for j, (i, to) in enumerate(
            zip([0, 1, 2, 2, 2, 3], [place.to_core, place.to_y] + place.to_z[1:] + [place.to_x])
        )
    ]

    def when(point):
        return pl.when(t == point)

    @when(0)
    def _():
        start(fetch_layer, operands(1), fetch_work, fetch_fold, fetch_gbt, operands(0))
        start(fetch, fetch_a1t)
        place.greet()
        fetch_work.wait()
        start(seg1.y[1])
        fetch_layer.wait()
        layer.send(0)
        fetch_fold.wait()
        start(seg1.z[0][:2])
        bqv_ref[...] = jnp.zeros_like(bqv_ref)
        sums_ref[0] = early_ref[...]
        fetch_gbt.wait()

    def wait(copies):
        for copy in copies:
            copy.wait()

    @when(0)
    def _():
        wait(operands(1))

    @when(4)
    def _():
        start(operands(3))
        wait(operands(0))

    @when(8)
    def _():
        start(operands(2))
        wait(operands(3))

    @when(9)
    def _():
        wait(operands(2))

    plan = [
        (1, 1, lambda: start(seg2.y[1][:2], seg2.z[0][:2])),
        (2, 1, lambda: (seg1.fold_y(1, 0), seg1.fold_z(0), start(seg2.y[1][2:]))),
        (3, 1, lambda: (layer.pass_on(0), layer.send(1))),
        (4, 1, lambda: seg1.fold_y(1, 1)),
        (5, 1, lambda: (seg1.fold_z(1), seg2.fold_z(0), seg2.fold_y(1, 0), layer.send(2))),
        (6, 1, lambda: layer.pass_on(1)),
        (7, 1, lambda: layer.send(3)),
        (8, 0, lambda: (seg2.fold_y(1, 1), layer.pass_on(2))),
        (8, 1, lambda: seg1.send_x()),
        (9, 1, lambda: (seg2.fold_z(1), seg0.fold_y(0, 0), layer.pass_on(3))),
        (11, 1, lambda: (seg2.send_x(), seg0.fold_y(0, 1))),
        (13, 1, lambda: (seg0.fold_z(0), out.pass_on(3))),
    ]

    def serve(point):
        for at, where, act in plan:
            if where == point:
                pl.when(t == at)(lambda act=act: (act(), None)[1])

    @pl.when((t == 0) | (t == 4) | (t == 8) | (t == 9))
    def _():
        pick = (
            lax.broadcasted_iota(jnp.int32, (8, width), 1) // HEAD_DIM
            == lax.broadcasted_iota(jnp.int32, (8, width), 0)
        ).astype(BF16)

        @pl.loop(0, n // step)
        def _(i):
            rows = pl.ds(pl.multiple_of(i * step, step), step)
            columns = scale_ref[now, :, rows].T
            lane = lax.broadcasted_iota(jnp.int32, (step, width), 1)
            scale = columns[:, heads - 1 : heads]
            for h in reversed(range(heads - 1)):
                scale = jnp.where(lane < (h + 1) * HEAD_DIM, columns[:, h : h + 1], scale)
            do = (dot_nn(gb_ref[rows, :], gw_ref[now]) * scale).astype(BF16)
            do_ref[now, rows, :] = do
            product = do.astype(F32) * o_ref[now, rows, :].astype(F32)
            high = product.astype(BF16)
            low = (product - high.astype(F32)).astype(BF16)
            delta_ref[now, :, rows] = dot_nt(pick, high) + dot_nt(pick, low)

        value = dot_nn(gbt_ref[...], o_ref[now]).astype(BF16)
        value = value.reshape(Z_DEV, Y_DEV, depth, width)

        hold_ref[now] = value

    serve(0)

    for ii in reversed(range(4)):
        @pl.when(i == ii)
        def _():
            first, last = ii * step, (ii + 1) * step
            do = do_ref[now, first:last, :]
            q = q_ref[now, first:last, :]
            v = v_ref[now, :last, :]
            lane = lax.broadcasted_iota(jnp.int32, (1, width), 1)
            dk, dv, dq = None, None, []
            for h in range(heads):
                low, high = h * HEAD_DIM, (h + 1) * HEAD_DIM
                here = (lane >= low) & (lane < high)
                p = p_ref[0, h, 0, :last, :]
                dp = dot_nt(v, jnp.where(here, do, jnp.zeros((), BF16)))
                ds = p * (dp - delta_ref[now, h : h + 1, first:last]).astype(BF16)
                part = dot_nn(p, do)
                dv = part if dv is None else jnp.where(lane < low, dv, part)
                part = dot_nn(ds, q)
                dk = part if dk is None else jnp.where(lane < low, dk, part)
                dq.append(dot_nn(kt_ref[now, low:high, :last], ds))
            if ii == 3:
                dkv_ref[now, 0] = dk
                dkv_ref[now, 1] = dv
            else:
                dkv_ref[now, 0, :last, :] += dk
                dkv_ref[now, 1, :last, :] += dv
            dk = dkv_ref[now, 0, first:last, :].astype(BF16)
            dv = dkv_ref[now, 1, first:last, :].astype(BF16)
            dq = (jnp.concatenate(dq, 0) * HEAD_DIM ** -0.5).astype(BF16).T
            dqkv_ref[now, first:last, :width] = dq
            dqkv_ref[now, first:last, width : 2 * width] = dk
            dqkv_ref[now, first:last, 2 * width :] = dv
            bqv_ref[mine, 0:1, :] += jnp.sum(dq.astype(F32), 0, keepdims=True)
            bqv_ref[mine, 1:2, :] += jnp.sum(dv.astype(F32), 0, keepdims=True)

            @pl.when(t >= 8)
            def _():
                da1_ref[first:last, :] += dot_nt(dqkv_ref[now, first:last, :], gq_ref[now])

    serve(1)

    @pl.when((t == 3) | (t == 7) | (t > 13))
    def _():
        @when(3)
        def _():
            fetch.wait()
            fetch_a1t.wait()

        @when(3)
        def _():
            da1_ref[...] = dot_nt(dqkv_ref[now], gq_ref[now])

        @when(7)
        def _():
            da1_ref[...] += dot_nt(dqkv_ref[now], gq_ref[now])

        value = dot_nn(a1t_ref[...], dqkv_ref[now]).reshape(Z_DEV, Y_DEV, depth, 3 * width)
        value = jnp.concatenate([value, hold_ref[now].astype(F32)], -1)
        for s in range(2):
            @when(3 + 11 * s)
            def _():
                if s:
                    core0[0].wait_send()
                stage0_ref[...] = value.astype(BF16)
                start(core0[s])

            @when(7 + 8 * s)
            def _():
                recv(core0[s])
                work0_ref[s] = (value + land0_ref[s].astype(F32)).astype(BF16)
                start(seg0.y[s])

    @pl.when((t > 8) & (t % 2 == 1))
    def _():
        rows = pl.ds(pl.multiple_of(i * step, step), step)
        xhat, r = norm_parts(own_ref[rows, :].astype(F32))
        da1 = da1_ref[rows, :]
        sums_ref[0, 0:1, :] += jnp.sum(da1 * xhat, 0, keepdims=True)
        sums_ref[0, 2:3, :] += jnp.sum(da1, 0, keepdims=True)
        dg = da1 * rows_ref[0:1, :]
        dv = r * (
            dg
            - jnp.mean(dg, -1, keepdims=True)
            - xhat * jnp.mean(dg * xhat, -1, keepdims=True)
        )
        own_ref[rows, :] = (dh1_ref[...] + dv).astype(BF16)
        for ii in range(4):
            @pl.when(i == ii)
            def _():
                out.send(ii)

    @when(15)
    def _():
        for s in range(4):
            sums_ref[0, 3:5, s * width : (s + 1) * width] = bqv_ref[s, 0:2, :]
        start(sum_core)
        out.pass_on(2)
        recv(sum_core)
        sums_ref[1] = sums_ref[0] + sumland_ref[0]
        start(sum_y)
        seg0.fold_y(1, 0)
        out.pass_on(1)
        seg0.fold_y(1, 1)
        recv(sum_y)
        sums_ref[2] = sums_ref[1] + sumland_ref[1]
        start(sum_z)
        seg0.fold_z(1)
        recv(sum_z)
        sums_ref[3] = (sums_ref[2] + sumland_ref[2]) + (sumland_ref[3] + sumland_ref[4])
        start(sum_x)
        part1_ref[...] = seg1.total()
        part2_ref[...] = seg2.total()
        seg0.send_x()
        layer.finish()
        out.pass_on(0)
        recv(sum_x)
        total_ref[...] = sums_ref[3] + sumland_ref[5]
        part0_ref[...] = seg0.total()
        out.finish()
        links.sent(core0[0])


def group_and_block(t):
    early = t < 8
    return (
        jnp.where(early, 1 - t // 4, 3 - t % 2),
        3 - jnp.where(early, t % 4, jnp.maximum(t - 8, 0) // 2),
    )


def run_fused_backward(
    tokens, gq, gw, rows, dh1, gb, gbt, q, v, kt, p, scale, o, a1t, layer, fold, work, early
):
    groups, n, _ = tokens.shape
    width = gw.shape[-1]
    heads = width // HEAD_DIM
    hidden = fold.shape[-1]
    depth = D // (Z_DEV * Y_DEV)
    step = n // 4

    p_spec = pl.BlockSpec(
        (1, heads, 1, n, step),
        lambda t: (group_and_block(t)[0], 0, group_and_block(t)[1], 0, 0),
    )

    copies = 2 * 12 + 2 + 15 + 2 * 11 + 6

    def landing(lanes, slots=1):
        return [
            pltpu.VMEM((slots, Z_DEV, depth, lanes), BF16),
            pltpu.VMEM((2, 3, depth, lanes), BF16), pltpu.VMEM((2, 2, depth, lanes), BF16),
            pltpu.VMEM((depth, lanes), BF16), pltpu.VMEM((depth, lanes), BF16),
        ]

    def working(lanes):
        block = (Z_DEV, Y_DEV, depth, lanes)
        return [pltpu.VMEM(block, BF16)] + [pltpu.VMEM((2,) + block, BF16)] * 2

    return pl.pallas_call(
        fused_backward,
        grid=(4 * groups,),
        in_specs=[
            ANY_WHOLE, ANY_WHOLE, ANY_WHOLE, VMEM_WHOLE,
            pl.BlockSpec((step, D), lambda t: (group_and_block(jnp.maximum(t, 8))[1], 0)),
            VMEM_WHOLE, ANY_WHOLE, ANY_WHOLE, ANY_WHOLE, ANY_WHOLE, p_spec,
            ANY_WHOLE, ANY_WHOLE, ANY_WHOLE, ANY_WHOLE, ANY_WHOLE, ANY_WHOLE, VMEM_WHOLE,
        ],
        out_specs=[ANY_WHOLE] * 2 + [VMEM_WHOLE] * 4,
        out_shape=[
            shaped(BF16, groups, n, D), shaped(BF16, groups, n, D),
            shaped(F32, depth, 4 * width), shaped(F32, depth, hidden),
            shaped(F32, depth, hidden), shaped(F32, 16, D),
        ],
        scratch_shapes=[
            pltpu.VMEM((2, D, 3 * width), BF16), pltpu.VMEM((2, D, width), BF16),
            pltpu.VMEM((2, n, width), BF16), pltpu.VMEM((2, n, width), BF16),
            pltpu.VMEM((2, width, n), BF16), pltpu.VMEM((2, 8, n), F32),
            pltpu.VMEM((2, n, width), BF16),
            pltpu.VMEM((D, n), BF16), pltpu.VMEM((D, n), BF16), pltpu.VMEM((n, D), BF16),
            pltpu.VMEM((2, Z_DEV, depth, hidden), BF16),
            pltpu.VMEM((2, Z_DEV, Y_DEV, depth, hidden), BF16),
            pltpu.VMEM((2, n, width), BF16),
            pltpu.VMEM((2, 8, n), F32), pltpu.VMEM((2, 2, n, width), F32),
            pltpu.VMEM((2, n, 3 * width), BF16),
            pltpu.VMEM((2, Z_DEV, Y_DEV, depth, width), BF16), pltpu.VMEM((n, D), F32),
            pltpu.VMEM((n, D), BF16), pltpu.VMEM((n, D), BF16), pltpu.VMEM((n, D), BF16),
            pltpu.VMEM((groups, 8, width), F32),
        ]
        + [pltpu.VMEM((2, Z_DEV, depth, hidden), BF16)] + landing(hidden) + landing(hidden)
        + working(4 * width) + landing(4 * width, 2)
        + [
            pltpu.VMEM((4, 16, D), F32), pltpu.VMEM((6, 16, D), F32),
            pltpu.SemaphoreType.DMA((copies,)), pltpu.SemaphoreType.DMA((copies,)),
            pltpu.SemaphoreType.DMA((6,)), pltpu.SemaphoreType.DMA((2, 2, 4)),
            pltpu.SemaphoreType.DMA((2, 7)),
        ],
        compiler_params=pltpu.CompilerParams(
            vmem_limit_bytes=VMEM_LIMIT, collective_id=2, has_side_effects=True
        ),
        name="fused_backward",
    )(tokens, gq, gw, rows, dh1, gb, gbt, q, v, kt, p, scale, o, a1t, layer, fold, work, early)


def place_gradients(
    tie_ref, sums_ref, part0_ref, part1_ref, part2_ref, near_out_ref,
    near_grad_ref, far_out_ref, far_grad_ref, gains_ref, bias_ref, in_ref, out_ref, expand_ref,
    project_ref, chosen_ref,
):
    t = pl.program_id(0)
    far_out_ref[...] = near_out_ref[...]
    far_grad_ref[...] = near_grad_ref[...]
    own = gains_ref.shape[-1]
    width = part0_ref.shape[-1] // 4
    kinds = [tie_ref[0], tie_ref[1], tie_ref[2], tie_ref[3]]

    @pl.when(t == 0)
    def _():
        first = (lax.axis_index("dp") * 4 + lax.axis_index("tensor")) * own
        feature = lax.broadcasted_iota(jnp.int32, (D, 128), 0)
        lane = lax.broadcasted_iota(jnp.int32, (D, 128), 1)
        chosen = ((feature == first + lane) & (lane < own)).astype(F32)
        chosen_ref[...] = lax.dot_general(
            sums_ref[...], chosen, (((1,), (0,)), ((), ())),
            precision=lax.Precision.HIGHEST, preferred_element_type=F32,
        )
        row = lax.broadcasted_iota(jnp.int32, (NSRC, own), 0)
        for i, kind in enumerate([0, 0, 0, 1, 2, 3, 2, 2, 2, 2]):
            value = chosen_ref[2 + i : 3 + i, :own]
            bias_ref[i] = jnp.where(row == kinds[kind], value, 0.0)

    @pl.when(t < NSRC)
    def _():
        def here(kind, value):
            return jnp.where(kinds[kind] == t, value, jnp.zeros_like(value))

        gains_ref[0, 0:1] = here(0, chosen_ref[0:1, :own])
        gains_ref[0, 1:2] = here(2, chosen_ref[1:2, :own])
        for j in range(3):
            in_ref[0, j] = here(0, part0_ref[:, j * width : (j + 1) * width])
        out_ref[0] = here(1, part0_ref[:, 3 * width :].T)
        expand_ref[0] = here(2, part1_ref[...])
        project_ref[0] = here(3, part2_ref[...])


def run_place_gradients(tie, sums, part0, part1, part2, out, grad, like):
    slots, n, _ = grad.shape
    gains, biases, w_in, w_out, w_expand, w_project = [item.shape for item in like]
    shapes = [
        gains, (biases[1], biases[0], biases[2]), w_in, w_out, w_expand,
        (w_project[0], w_project[2], w_project[1]),
    ]

    def source(shape):
        return pl.BlockSpec(
            (1,) + shape[1:], lambda t: (jnp.minimum(t, NSRC - 1),) + (0,) * (len(shape) - 1)
        )

    out, grad, gains, biases, w_in, w_out, w_expand, w_project = pl.pallas_call(
        place_gradients,
        grid=(slots,),
        in_specs=[SMEM_WHOLE] + [VMEM_WHOLE] * 4 + [group(n, D), group(n, D)],
        out_specs=[group(n, D), group(n, D), source(shapes[0]), VMEM_WHOLE]
        + [source(shape) for shape in shapes[2:]],
        out_shape=[shaped(BF16, slots, n, D)] * 2 + [shaped(F32, *item) for item in shapes],
        scratch_shapes=[pltpu.VMEM((16, 128), F32)],
        compiler_params=pltpu.CompilerParams(vmem_limit_bytes=VMEM_LIMIT),
        name="place_gradients",
    )(tie, sums, part0, part1, part2, out, grad)
    biases = biases.transpose(1, 0, 2)
    return out, grad, gains, biases, w_in, w_out, w_expand, w_project.transpose(0, 2, 1)


def plain_step(
    tokens, lengths, tie_map, norm_gains, bias_rows, attention_in, attention_out,
    expand_weight, project_weight, cotangent,
):
    slot_rows = tokens.shape[0] // lengths.shape[0]
    me = lax.axis_index("tensor")
    in_local = lax.dynamic_index_in_dim(attention_in, tie_map[0], 0, keepdims=False)
    out_local = lax.dynamic_index_in_dim(attention_out, tie_map[1], 0, keepdims=False)
    expand_local = lax.dynamic_index_in_dim(expand_weight, tie_map[2], 0, keepdims=False)
    project_local = lax.dynamic_index_in_dim(project_weight, tie_map[3], 0, keepdims=False)
    local0 = jnp.concatenate([in_local, out_local.T[None]], 0)
    row_kinds = jnp.array([0, 0, 0, 1, 2, 3] + [2] * (FF // D), dtype=jnp.int32)
    gain_kinds = jnp.array([0, 2], dtype=jnp.int32)
    gain_pick = norm_gains[tie_map[gain_kinds], jnp.arange(2)]
    bias_pick = bias_rows[tie_map[row_kinds], jnp.arange(row_kinds.shape[0])]
    vectors = jnp.concatenate([gain_pick, bias_pick], 0)
    x = lax.dynamic_slice_in_dim(tokens, me * slot_rows, slot_rows, 0)
    cot = lax.dynamic_slice_in_dim(cotangent, me * slot_rows, slot_rows, 0)
    length = lax.dynamic_slice_in_dim(lengths, me, 1, 0)
    rows = lax.all_gather(vectors, ("dp", "tensor"), axis=1, tiled=True).astype(F32)
    rows = jnp.concatenate([rows, jnp.zeros((4, D), F32)], 0)

    def gathered(piece, axis):
        piece = lax.all_gather(piece, "dp", axis=axis, tiled=True)
        return lax.all_gather(piece, "tensor", axis=0)

    g0 = gathered(local0, 1)
    g1 = gathered(expand_local, 0)
    g2 = gathered(project_local.T, 0)
    groups, width = g0.shape[0], g0.shape[-1]
    bqv = rows[3:5].reshape(2, groups, width).transpose(1, 0, 2)
    q, v, kt, p, o, a1t, h1, a2, a2t = run_attention_forward(length, x, g0, rows, bqv)
    out, d1, d2, dh1, gb, gbt, sums = run_feed_forward(length, cot, a2, a2t, h1, g1, g2, rows)
    d0, xg, sums_in, sums_qv = run_attention_backward(
        x, g0, rows, dh1, gb, gbt, q, v, kt, p, o, a1t
    )
    layer_out = lax.all_gather(out, "tensor", axis=0, tiled=True)
    tokens_grad = lax.all_gather(xg, "tensor", axis=0, tiled=True)

    def scattered(piece, axis):
        piece = lax.psum_scatter(piece, "tensor", scatter_dimension=0)
        return lax.psum_scatter(piece, "dp", scatter_dimension=axis, tiled=True).astype(F32)

    part0 = scattered(d0, 1)
    part1 = scattered(d1, 0)
    part2 = scattered(d2, 0)
    qv = sums_qv[:, :2].transpose(1, 0, 2).reshape(2, D)
    sums = jnp.concatenate(
        [sums_in[0:1], sums[1:2], sums_in[1:2], qv, sums[5:12]], 0
    )
    sums = lax.psum_scatter(sums, ("dp", "tensor"), scatter_dimension=1, tiled=True)
    return layer_out, tokens_grad, *placed(tie_map, sums, part0, part1, part2)


def fused_step(
    tokens, lengths, tie_map, norm_gains, bias_rows, attention_in, attention_out,
    expand_weight, project_weight, cotangent,
):
    slots = lengths.shape[0]
    tokens = tokens.reshape(slots, -1, D)
    cotangent = cotangent.reshape(slots, -1, D)
    gq, gw, g1, g2, rows, q, v, kt, p, scale, o, a1t, h1, a2, a2t = run_fused_forward(
        tie_map, lengths, tokens, norm_gains, bias_rows, attention_in, attention_out,
        expand_weight, project_weight,
    )
    layer, fold, work, dh1, gb, gbt, early = run_fused_feed_forward(
        lengths, cotangent, a2, a2t, h1, g1, g2, rows
    )
    grad, out, part0, part1, part2, sums = run_fused_backward(
        tokens, gq, gw, rows, dh1, gb, gbt, q, v, kt, p, scale, o, a1t, layer, fold,
        work, early,
    )
    out, grad, *placed_grads = run_place_gradients(
        tie_map, sums, part0, part1, part2, out, grad,
        (norm_gains, bias_rows, attention_in, attention_out, expand_weight, project_weight),
    )
    return out.reshape(-1, D), grad.reshape(-1, D), *placed_grads


def placed(tie_map, sums, part0, part1, part2):
    source = jnp.arange(NSRC, dtype=jnp.int32)

    def place(piece, which):
        pick = (source == tie_map[which]).reshape((NSRC,) + (1,) * piece.ndim)
        return jnp.where(pick, piece[None], 0.0)

    def place_rows(piece, kinds):
        pick = source[:, None] == tie_map[jnp.array(kinds, dtype=jnp.int32)][None, :]
        return jnp.where(pick[:, :, None], piece[None], 0.0)

    return (
        place_rows(sums[:2], [0, 2]),
        place_rows(sums[2:], [0, 0, 0, 1, 2, 3] + [2] * (FF // D)),
        place(part0[:3], 0),
        place(part0[3].T, 1),
        place(part1, 2),
        place(part2.T, 3),
    )


def solution(mesh):
    fused = mesh.shape["dp"] == Z_DEV * Y_DEV and mesh.shape["tensor"] == X_DEV * C_DEV
    return jax.shard_map(
        fused_step if fused else plain_step,
        mesh=mesh,
        in_specs=(
            P("dp", None),
            P("dp"),
            P(),
            P(None, None, ("dp", "tensor")),
            P(None, None, ("dp", "tensor")),
            P(None, None, "dp", "tensor"),
            P(None, "tensor", "dp"),
            P(None, "dp", "tensor"),
            P(None, "tensor", "dp"),
            P("dp", None),
        ),
        out_specs=(
            P("dp", None),
            P("dp", None),
            P(None, None, ("dp", "tensor")),
            P(None, None, ("dp", "tensor")),
            P(None, None, "dp", "tensor"),
            P(None, "tensor", "dp"),
            P(None, "dp", "tensor"),
            P(None, "tensor", "dp"),
        ),
        check_vma=False,
    )
```

```python
import jax
import jax.numpy as jnp
from jax import lax
from jax.experimental import pallas as pl
from jax.experimental.pallas import tpu as pltpu
from jax.sharding import PartitionSpec as P

D = 768
HEAD_DIM = 64
FF = 3072
NSRC = 4
EPS = 1e-05
MASKED = -1e30
F32 = jnp.float32
BF16 = jnp.bfloat16
VMEM_LIMIT = 60 * 1024 * 1024


def dot_nn(a, b):
    return lax.dot_general(a, b, (((1,), (0,)), ((), ())), preferred_element_type=F32)


def dot_nt(a, b):
    return lax.dot_general(a, b, (((1,), (1,)), ((), ())), preferred_element_type=F32)


def norm_parts(v):
    center = jnp.mean(v, -1, keepdims=True)
    centered = v - center
    r = lax.rsqrt(jnp.mean(centered * centered, -1, keepdims=True) + EPS)
    return centered * r, r


def head_mask(shape, h):
    lane = lax.broadcasted_iota(jnp.int32, shape, 1)
    return (lane >= h * HEAD_DIM) & (lane < (h + 1) * HEAD_DIM)


def blocks(total, size):
    return [slice(i * size, (i + 1) * size) for i in range(total // size)]


def attention_forward(
    len_ref, x_ref, g_ref, rows_ref, bqv_ref,
    q_ref, v_ref, kt_ref, p_ref, o_ref, a1t_ref, h1_ref, a2_ref, a2t_ref,
    a1_ref, k_ref, vt_ref, ot_ref, attn_ref,
):
    t = pl.program_id(0)
    n = x_ref.shape[0]
    width = g_ref.shape[-1]
    heads = width // HEAD_DIM
    step = 256
    length = len_ref[0]

    @pl.when(t == 0)
    def _():
        @pl.loop(0, n // step)
        def _(b):
            rows = pl.ds(pl.multiple_of(b * step, step), step)
            xhat, _ = norm_parts(x_ref[rows, :].astype(F32))
            a1 = xhat * rows_ref[0:1, :] + rows_ref[2:3, :]
            a1_ref[rows, :] = a1.astype(BF16)
            a1t_ref[:, rows] = a1.astype(BF16).T
            attn_ref[rows, :] = x_ref[rows, :].astype(F32) + rows_ref[5:6, :]

    @pl.loop(0, n // step)
    def _(b):
        rows = pl.ds(pl.multiple_of(b * step, step), step)
        a1 = a1_ref[rows, :]
        q = (dot_nn(a1, g_ref[0, 0]) + bqv_ref[0, 0:1, :]).astype(BF16)
        q_ref[0, rows, :] = q * jnp.asarray(HEAD_DIM ** -0.5, BF16)
        k = dot_nn(a1, g_ref[0, 1]).astype(BF16)
        k_ref[rows, :] = k
        kt_ref[0, :, rows] = k.T
        v = (dot_nn(a1, g_ref[0, 2]) + bqv_ref[0, 1:2, :]).astype(BF16)
        v_ref[0, rows, :] = v
        vt_ref[:, rows] = v.T

    for h in range(heads):
        k = k_ref[...]
        k = jnp.where(head_mask(k.shape, h), k, jnp.zeros_like(k))
        for b in range(n // step):
            first, last = b * step, (b + 1) * step
            q = q_ref[0, first:last, :]
            key = lax.broadcasted_iota(jnp.int32, (last, step), 0)
            query = lax.broadcasted_iota(jnp.int32, (step, step), 1) + first
            s = dot_nt(k[:last], q)
            near = jnp.where(
                (key[first:] <= query) & (key[first:] < length), s[first:], MASKED
            )
            if b:
                far = jnp.where(key[:first] < length, s[:first], MASKED)
                top = jnp.maximum(
                    jnp.max(far, 0, keepdims=True), jnp.max(near, 0, keepdims=True)
                )
                e_far = jnp.exp(far - top)
                e_near = jnp.exp(near - top)
                total = jnp.sum(e_far, 0, keepdims=True) + jnp.sum(e_near, 0, keepdims=True)
                scale = 1.0 / total
                p_ref[0, h, :first, first:last] = (e_far * scale).astype(BF16)
            else:
                top = jnp.max(near, 0, keepdims=True)
                e_near = jnp.exp(near - top)
                scale = 1.0 / jnp.sum(e_near, 0, keepdims=True)
            p_ref[0, h, first:last, first:last] = (e_near * scale).astype(BF16)
            ot_ref[h * HEAD_DIM : (h + 1) * HEAD_DIM, first:last] = dot_nn(
                vt_ref[h * HEAD_DIM : (h + 1) * HEAD_DIM, :last],
                p_ref[0, h, :last, first:last],
            ).astype(BF16)

    @pl.loop(0, n // step)
    def _(b):
        rows = pl.ds(pl.multiple_of(b * step, step), step)
        o = ot_ref[:, rows].T
        o_ref[0, rows, :] = o
        attn_ref[rows, :] += dot_nt(o, g_ref[0, 3])

    @pl.when(t == pl.num_programs(0) - 1)
    def _():
        @pl.loop(0, n // step)
        def _(b):
            rows = pl.ds(pl.multiple_of(b * step, step), step)
            h1 = attn_ref[rows, :]
            h1_ref[rows, :] = h1
            xhat, _ = norm_parts(h1)
            a2 = (xhat * rows_ref[1:2, :] + rows_ref[6:7, :]).astype(BF16)
            a2_ref[rows, :] = a2
            a2t_ref[:, rows] = a2.T


SQRT_2_PI = 0.7978845608028654


def feed_forward_both(
    len_ref, c_ref, a2_ref, a2t_ref, h1_ref, w1_ref, w2_ref, rows_ref,
    out_ref, d1_ref, d2_ref, dh1_ref, gb_ref, gbt_ref, sums_ref,
    gf_ref, gft_ref, feed_ref, da2_ref, h_ref, df_ref,
):
    t = pl.program_id(0)
    n = c_ref.shape[0]
    step = 256
    length = len_ref[0]

    @pl.when(t == 0)
    def _():
        sums_ref[...] = jnp.zeros_like(sums_ref)

        @pl.loop(0, n // step)
        def _(b):
            rows = pl.ds(pl.multiple_of(b * step, step), step)
            place = b * step + lax.broadcasted_iota(jnp.int32, (step, 1), 0)
            live = (place < length).astype(F32)
            g = (c_ref[rows, :].astype(F32) * live).astype(BF16)
            gf_ref[rows, :] = g
            gft_ref[:, rows] = g.T
            sums_ref[7:8, :] += jnp.sum(g.astype(F32), 0, keepdims=True)

    bias = rows_ref[pl.ds(8 + t, 1), :]

    @pl.loop(0, n // step)
    def _(b):
        rows = pl.ds(pl.multiple_of(b * step, step), step)
        f = dot_nn(a2_ref[rows, :], w1_ref[0]) + bias
        dh = dot_nn(gf_ref[rows, :], w2_ref[0])
        f2 = f * f
        th = jnp.tanh(f * (SQRT_2_PI + (SQRT_2_PI * 0.044715) * f2))
        half = 0.5 + 0.5 * th
        h = (f * half).astype(BF16)
        slope = half + f * (0.5 - 0.5 * th * th) * (
            SQRT_2_PI + (3 * SQRT_2_PI * 0.044715) * f2
        )
        df = (dh * slope).astype(BF16)
        h_ref[rows, :] = h
        df_ref[rows, :] = df
        sums_ref[pl.ds(8 + t, 1), :] += jnp.sum(df.astype(F32), 0, keepdims=True)
        feed = dot_nt(h, w2_ref[0])
        da2 = dot_nt(df, w1_ref[0])

        @pl.when(t == 0)
        def _():
            feed_ref[rows, :] = feed
            da2_ref[rows, :] = da2

        @pl.when(t > 0)
        def _():
            feed_ref[rows, :] += feed
            da2_ref[rows, :] += da2

    @pl.loop(0, D // step)
    def _(b):
        rows = pl.ds(pl.multiple_of(b * step, step), step)
        d1_ref[0, rows, :] = dot_nn(a2t_ref[rows, :], df_ref[...]).astype(BF16)
        d2_ref[0, rows, :] = dot_nn(gft_ref[rows, :], h_ref[...]).astype(BF16)

    @pl.when(t == pl.num_programs(0) - 1)
    def _():
        @pl.loop(0, n // step)
        def _(b):
            rows = pl.ds(pl.multiple_of(b * step, step), step)
            place = b * step + lax.broadcasted_iota(jnp.int32, (step, 1), 0)
            live = (place < length).astype(F32)
            h1 = h1_ref[rows, :]
            out_ref[rows, :] = (live * (h1 + (feed_ref[rows, :] + rows_ref[7:8, :]))).astype(BF16)
            xhat, r = norm_parts(h1)
            da2 = da2_ref[rows, :]
            sums_ref[1:2, :] += jnp.sum(da2 * xhat, 0, keepdims=True)
            sums_ref[6:7, :] += jnp.sum(da2, 0, keepdims=True)
            dg = da2 * rows_ref[1:2, :]
            dv = r * (
                dg
                - jnp.mean(dg, -1, keepdims=True)
                - xhat * jnp.mean(dg * xhat, -1, keepdims=True)
            )
            dh1 = live * c_ref[rows, :].astype(F32) + dv
            dh1_ref[rows, :] = dh1
            gb = dh1.astype(BF16)
            gb_ref[rows, :] = gb
            gbt_ref[:, rows] = gb.T
            sums_ref[5:6, :] += jnp.sum(gb.astype(F32), 0, keepdims=True)


def attention_backward(
    x_ref, g_ref, rows_ref, dh1_ref, gb_ref, gbt_ref, q_ref, v_ref, kt_ref, p_ref,
    o_ref, a1t_ref,
    d0_ref, xg_ref, sums_ref, bqv_ref,
    do_ref, delta_ref, dqt_ref, dq_ref, dk_ref, dv_ref, da1_ref,
):
    t = pl.program_id(0)
    n = x_ref.shape[0]
    width = g_ref.shape[-1]
    heads = width // HEAD_DIM
    step = 256
    pick = (
        lax.broadcasted_iota(jnp.int32, (16, width), 1) // HEAD_DIM
        == lax.broadcasted_iota(jnp.int32, (16, width), 0)
    ).astype(BF16)

    @pl.loop(0, n // step)
    def _(b):
        rows = pl.ds(pl.multiple_of(b * step, step), step)
        do = dot_nn(gb_ref[rows, :], g_ref[0, 3]).astype(BF16)
        do_ref[rows, :] = do
        prod = do.astype(F32) * o_ref[0, rows, :].astype(F32)
        high = prod.astype(BF16)
        low = (prod - high.astype(F32)).astype(BF16)
        delta_ref[:, rows] = dot_nt(pick, high) + dot_nt(pick, low)

    dqt_ref[...] = jnp.zeros_like(dqt_ref)
    for b in range(n // step):
        first, last = b * step, (b + 1) * step
        do = do_ref[first:, :]
        q = q_ref[0, first:, :]
        v = v_ref[0, first:last, :]
        dk, dv = None, None
        for h in range(heads):
            mine = head_mask((1, width), h)
            zero = jnp.zeros((), BF16)
            p = p_ref[0, h, first:last, first:]
            dp = dot_nt(jnp.where(mine, v, zero), do)
            ds = (p.astype(F32) * (dp - delta_ref[h : h + 1, first:])).astype(BF16)
            part = dot_nn(p, jnp.where(mine, do, zero))
            dv = part if dv is None else dv + part
            part = dot_nn(ds, jnp.where(mine, q, zero))
            dk = part if dk is None else dk + part
            head = slice(h * HEAD_DIM, (h + 1) * HEAD_DIM)
            dqt_ref[head, first:] += dot_nn(kt_ref[0, head, first:last], ds)
        dk_ref[first:last, :] = dk.astype(BF16)
        dv_ref[first:last, :] = dv.astype(BF16)

    @pl.when(t == 0)
    def _():
        da1_ref[...] = jnp.zeros_like(da1_ref)

    bqv_ref[...] = jnp.zeros_like(bqv_ref)

    @pl.loop(0, n // step)
    def _(b):
        rows = pl.ds(pl.multiple_of(b * step, step), step)
        dq = (dqt_ref[:, rows] * HEAD_DIM ** -0.5).astype(BF16).T
        dk = dk_ref[rows, :]
        dv = dv_ref[rows, :]
        dq_ref[rows, :] = dq
        bqv_ref[0, 0:1, :] += jnp.sum(dq.astype(F32), 0, keepdims=True)
        bqv_ref[0, 1:2, :] += jnp.sum(dv.astype(F32), 0, keepdims=True)
        da1_ref[rows, :] += (
            dot_nt(dq, g_ref[0, 0]) + dot_nt(dk, g_ref[0, 1]) + dot_nt(dv, g_ref[0, 2])
        )

    @pl.loop(0, D // step)
    def _(b):
        rows = pl.ds(pl.multiple_of(b * step, step), step)
        a1t = a1t_ref[rows, :]
        d0_ref[0, 0, rows, :] = dot_nn(a1t, dq_ref[...]).astype(BF16)
        d0_ref[0, 1, rows, :] = dot_nn(a1t, dk_ref[...]).astype(BF16)
        d0_ref[0, 2, rows, :] = dot_nn(a1t, dv_ref[...]).astype(BF16)
        d0_ref[0, 3, rows, :] = dot_nn(gbt_ref[rows, :], o_ref[0]).astype(BF16)

    @pl.when(t == pl.num_programs(0) - 1)
    def _():
        sums_ref[...] = jnp.zeros_like(sums_ref)

        @pl.loop(0, n // step)
        def _(b):
            rows = pl.ds(pl.multiple_of(b * step, step), step)
            xhat, r = norm_parts(x_ref[rows, :].astype(F32))
            da1 = da1_ref[rows, :]
            sums_ref[0:1, :] += jnp.sum(da1 * xhat, 0, keepdims=True)
            sums_ref[1:2, :] += jnp.sum(da1, 0, keepdims=True)
            dg = da1 * rows_ref[0:1, :]
            dv = r * (
                dg
                - jnp.mean(dg, -1, keepdims=True)
                - xhat * jnp.mean(dg * xhat, -1, keepdims=True)
            )
            xg_ref[rows, :] = (dh1_ref[rows, :] + dv).astype(BF16)


def whole(*shape):
    return pl.BlockSpec(shape, lambda t: (0,) * len(shape))


def group(*shape):
    return pl.BlockSpec((1,) + shape, lambda t: (t,) + (0,) * len(shape))


def shaped(dtype, *shape):
    return jax.ShapeDtypeStruct(shape, dtype)


SMEM_WHOLE = pl.BlockSpec(memory_space=pltpu.SMEM)


def run_attention_forward(length, x, g0, rows, bqv):
    n = x.shape[0]
    groups, _, _, width = g0.shape
    heads = width // HEAD_DIM
    return pl.pallas_call(
        attention_forward,
        grid=(groups,),
        in_specs=[SMEM_WHOLE, whole(n, D), group(4, D, width), whole(16, D), group(2, width)],
        out_specs=[
            group(n, width), group(n, width), group(width, n), group(heads, n, n),
            group(n, width), whole(D, n), whole(n, D), whole(n, D), whole(D, n),
        ],
        out_shape=[
            shaped(BF16, groups, n, width), shaped(BF16, groups, n, width),
            shaped(BF16, groups, width, n), shaped(BF16, groups, heads, n, n),
            shaped(BF16, groups, n, width), shaped(BF16, D, n), shaped(F32, n, D),
            shaped(BF16, n, D), shaped(BF16, D, n),
        ],
        scratch_shapes=[
            pltpu.VMEM((n, D), BF16), pltpu.VMEM((n, width), BF16),
            pltpu.VMEM((width, n), BF16), pltpu.VMEM((width, n), BF16),
            pltpu.VMEM((n, D), F32),
        ],
        compiler_params=pltpu.CompilerParams(vmem_limit_bytes=VMEM_LIMIT),
        name="attention_forward",
    )(length, x, g0, rows, bqv)


def run_feed_forward(length, cot, a2, a2t, h1, g1, g2, rows):
    n = cot.shape[0]
    groups, _, width = g1.shape
    return pl.pallas_call(
        feed_forward_both,
        grid=(groups,),
        in_specs=[
            SMEM_WHOLE, whole(n, D), whole(n, D), whole(D, n), whole(n, D),
            group(D, width), group(D, width), whole(16, D),
        ],
        out_specs=[
            whole(n, D), group(D, width), group(D, width), whole(n, D), whole(n, D),
            whole(D, n), whole(16, D),
        ],
        out_shape=[
            shaped(BF16, n, D), shaped(BF16, groups, D, width), shaped(BF16, groups, D, width),
            shaped(F32, n, D), shaped(BF16, n, D), shaped(BF16, D, n), shaped(F32, 16, D),
        ],
        scratch_shapes=[
            pltpu.VMEM((n, D), BF16), pltpu.VMEM((D, n), BF16), pltpu.VMEM((n, D), F32),
            pltpu.VMEM((n, D), F32), pltpu.VMEM((n, width), BF16), pltpu.VMEM((n, width), BF16),
        ],
        compiler_params=pltpu.CompilerParams(vmem_limit_bytes=VMEM_LIMIT),
        name="feed_forward_both",
    )(length, cot, a2, a2t, h1, g1, g2, rows)


def run_attention_backward(x, g0, rows, dh1, gb, gbt, q, v, kt, p, o, a1t):
    n = x.shape[0]
    groups, _, _, width = g0.shape
    heads = width // HEAD_DIM
    return pl.pallas_call(
        attention_backward,
        grid=(groups,),
        in_specs=[
            whole(n, D), group(4, D, width), whole(16, D), whole(n, D), whole(n, D),
            whole(D, n), group(n, width), group(n, width), group(width, n),
            group(heads, n, n), group(n, width), whole(D, n),
        ],
        out_specs=[group(4, D, width), whole(n, D), whole(8, D), group(8, width)],
        out_shape=[
            shaped(BF16, groups, 4, D, width), shaped(BF16, n, D), shaped(F32, 8, D),
            shaped(F32, groups, 8, width),
        ],
        scratch_shapes=[
            pltpu.VMEM((n, width), BF16), pltpu.VMEM((16, n), F32), pltpu.VMEM((width, n), F32),
            pltpu.VMEM((n, width), BF16), pltpu.VMEM((n, width), BF16),
            pltpu.VMEM((n, width), BF16), pltpu.VMEM((n, D), F32),
        ],
        compiler_params=pltpu.CompilerParams(vmem_limit_bytes=VMEM_LIMIT),
        name="attention_backward",
    )(x, g0, rows, dh1, gb, gbt, q, v, kt, p, o, a1t)


Z_DEV, Y_DEV, X_DEV, C_DEV = 4, 2, 2, 2


class Place:
    def __init__(self):
        dp, self.t = lax.axis_index("dp"), lax.axis_index("tensor")
        self.dp = dp
        self.z, self.y = dp // 2, dp % 2
        self.x, self.c = self.t // 2, self.t % 2
        self.other_y = 1 - self.y
        self.zs = [
            self.z,
            self.z + 1 - 2 * (self.z % 2),
            self.z + 2 - 4 * (self.z // 2),
            3 - self.z,
        ]
        self.ts = [
            self.t,
            self.t + 1 - 2 * (self.t % 2),
            self.t + 2 - 4 * (self.t // 2),
            3 - self.t,
        ]
        self.to_z = [dict(dp=z * 2 + self.y) for z in self.zs]
        self.to_y = dict(dp=self.z * 2 + self.other_y)
        self.to_x = dict(tensor=self.ts[2])
        self.same_t = self.to_z[1:] + [dict(dp=z * 2 + self.other_y) for z in self.zs]
        self.same_dp = [dict(tensor=t) for t in self.ts[1:]]
        self.to_core = dict(tensor=self.ts[1])

    def group(self, k):
        return lax.select(
            k == 0, self.ts[0],
            lax.select(k == 1, self.ts[1], lax.select(k == 2, self.ts[2], self.ts[3])),
        )

    def greet(self, others=None):
        barrier = pltpu.get_barrier_semaphore()
        others = others or self.to_z[1:] + [self.to_y, self.to_x, self.to_core]
        for device in others:
            pl.semaphore_signal(
                barrier, inc=1, device_id=device, device_id_type=pl.DeviceIdType.MESH
            )
        pl.semaphore_wait(barrier, len(others))


class Pieces:
    def __init__(self, whole, pieces):
        self.whole, self.pieces = whole, pieces

    def start(self):
        for piece in self.pieces:
            piece.start()

    def wait_recv(self):
        self.whole.wait_recv()

    def wait_send(self):
        self.whole.wait_send()


class Links:
    def __init__(self, send_sem, recv_sem):
        self.send_sem, self.recv_sem = send_sem, recv_sem
        self.copies = []

    def add(self, device, src, dst, parts=1, axis=0):
        number = len(self.copies)

        def make(src, dst):
            return pltpu.make_async_remote_copy(
                src_ref=src,
                dst_ref=dst,
                send_sem=self.send_sem.at[number],
                recv_sem=self.recv_sem.at[number],
                device_id=device,
                device_id_type=pl.DeviceIdType.MESH,
            )

        size = src.shape[axis] // parts
        cuts = [(slice(None),) * axis + (pl.ds(i * size, size),) for i in range(parts)]
        copy = Pieces(make(src, dst), [make(src.at[cut], dst.at[cut]) for cut in cuts])
        self.copies.append(copy)
        return copy

    def sent(self, *apart):
        for copy in self.copies:
            if all(copy is not other for other in apart):
                copy.wait_send()


def flat(copies):
    for item in copies:
        if isinstance(item, list):
            yield from flat(item)
        else:
            yield item


def start(*copies):
    for copy in flat(copies):
        copy.start()


def recv(*copies):
    for copy in flat(copies):
        copy.wait_recv()


class Gather:
    def __init__(self, links, place, own, full, order, single=True, last=True):
        every = slice(None)
        y, other = place.y, place.other_y

        def same(device, k, yy, to):
            return links.add(device, full(k, every, yy), full(to, every, yy), Z_DEV)

        def along_z(k, yy, block):
            here, passed = full(k, place.z, yy), full(k, place.zs[2], yy)
            return [
                links.add(place.to_z[1], block, here),
                links.add(place.to_z[2], block, here),
                links.add(place.to_z[1], passed, passed),
            ]

        if order != WHOLE:
            self.z = along_z(0, y, own)
        if order == X_Z_Y:
            self.first = [links.add(place.to_x, own, full(2, place.z, y), 2)]
            self.far = along_z(2, y, full(2, place.z, y))
            blocks = [(0, y), (2, y), (0, other), (2, other)]
        else:
            blocks = [(0, y), (0, other), (2, y), (2, other)]
        if order == Y_Z_X:
            self.first = [links.add(place.to_y, own, full(0, place.z, y), 2)]
            self.far = along_z(0, other, full(0, place.z, other))
        if order == Z_Y_X and single:
            self.first = [same(place.to_y, 0, y, 0)]
        if order == Z_Y_X and not single:
            self.first = [links.add(place.to_y, own, full(0, place.z, y))]
            for k in range(1, 4):
                block = full(0, place.zs[k], y)
                self.first.append(links.add(place.to_y, block, block))
            return
        self.second = [
            same(place.to_y, k, yy, k) if order == X_Z_Y else same(place.to_x, k, yy, 2)
            for k, yy in blocks[: 2 if last else 1]
        ]
        if not last:
            blocks = [block for block in blocks if block[0] == 0]
        self.core = [same(place.to_core, k, yy, k + 1) for k, yy in blocks]


Z_Y_X, Y_Z_X, X_Z_Y, WHOLE = range(4)


def fused_forward(
    tie_ref, len_ref, tokens_ref, gains_ref, bias_ref, in_ref, out_ref, expand_ref,
    project_ref,
    gq_ref, gw_ref, flat1_ref, flat2_ref, rows_ref,
    q_ref, v_ref, kt_ref, p_ref, scale_ref, o_ref, a1t_out, h1_out, a2_out, a2t_out,
    own0_ref, own1_ref, own2_ref, square_ref, vec_ref,
    all0_ref, w1_ref, w2_ref, vecs_ref, bqv_ref, x_ref, a1_ref, k_ref, qa_ref, vt_ref, ot_ref, a1t_ref, h1_ref, a2_ref, a2t_ref,
    send_sem, recv_sem, local_sem, flush_sem, row_sem,
):
    t, h = pl.program_id(0), pl.program_id(1)
    n, _ = x_ref.shape
    width = q_ref.shape[-1]
    heads = width // HEAD_DIM
    step = 256
    place = Place()
    length = len_ref[place.t]
    links = Links(send_sem, recv_sem)
    z, y, x, c = place.z, place.y, place.x, place.c
    mine_there = vecs_ref.at[z, y, x, c]
    column = vecs_ref.at[:, :, x, c]
    vec_one = [links.add(device, vec_ref, mine_there) for device in place.same_t]
    vec_two = [links.add(device, column, column) for device in place.same_dp]
    half = own0_ref.shape[0] // 2
    halves = []
    for i in range(2):
        rows = pl.ds(i * half, half)
        halves.append(Gather(
            links, place, own0_ref.at[rows],
            lambda k, z, y, rows=rows: all0_ref.at[k, z, y, rows], Z_Y_X, single=False,
        ))
    seg0 = Gather(links, place, own0_ref, lambda k, z, y: all0_ref.at[k, z, y], WHOLE)
    seg1 = Gather(
        links, place, own1_ref, lambda k, z, y: w1_ref.at[k, z, y], Y_Z_X, last=False
    )
    seg2 = Gather(
        links, place, own2_ref, lambda k, z, y: w2_ref.at[k, z, y], X_Z_Y, last=False
    )
    flush = [
        [
            pltpu.make_async_copy(ref.at[k], flat.at[k], flush_sem.at[i, k])
            for k in range(3)
        ]
        for i, (ref, flat) in enumerate([(w1_ref, flat1_ref), (w2_ref, flat2_ref)])
    ]
    put_a1t = pltpu.make_async_copy(a1t_ref, a1t_out, local_sem.at[0])
    put_a2t = pltpu.make_async_copy(a2t_ref, a2t_out, local_sem.at[1])
    puts = []
    for i in range(n // step):
        rows = pl.ds(i * step, step)
        puts.append([
            pltpu.make_async_copy(h1_ref.at[rows], h1_out.at[rows], row_sem.at[0, i]),
            pltpu.make_async_copy(a2_ref.at[rows], a2_out.at[rows], row_sem.at[1, i]),
        ])
    fetch = pltpu.make_async_copy(tokens_ref.at[place.t], x_ref, local_sem.at[2])

    def relay_z(copies):
        recv(copies[1])
        start(copies[2])

    def pass_own(seg):
        recv(seg.z[0], seg.z[2])
        start(seg.second[0], seg.core[0])

    def pass_second(seg):
        recv(seg.second)
        if seg is seg2:
            start(seg.core[1])

    def pass_first(seg):
        recv(seg.first)
        start(seg.far[1], seg.far[0])

    def pass_far(seg):
        recv(seg.far[0], seg.far[2])
        start(seg.core[1:] if seg is seg1 else [])

    def pass_core(seg, i):
        recv(seg.second[i])
        start(seg.core[2 + i])

    plan = [
        (0, 0, lambda: (pass_first(seg1), relay_z(seg2.z), pass_first(seg2))),
        (0, 3, lambda: (relay_z(seg1.z), pass_core(seg0, 0))),
        (1, 0, lambda: recv(seg0.core[:2])),
        (1, 1, lambda: relay_z(seg1.far)),
        (1, 3, lambda: pass_core(seg0, 1)),
        (1, 4, lambda: pass_own(seg2)),
        (2, 1, lambda: relay_z(seg2.far)),
        (2, 3, lambda: pass_own(seg1)),
        (3, 0, lambda: (recv(seg0.core[2:]), pass_far(seg1), flush[0][0].start())),
        (3, 2, lambda: (pass_second(seg2), flush[1][0].start())),
        (3, 3, lambda: (pass_far(seg2), flush[1][2].start())),
    ]

    def serve(points):
        for step, where, act in plan:
            if where in points:
                now = (t == step) & (h == max(where - 2, 0))
                pl.when(now)(lambda act=act: (act(), None)[1])

    @pl.when((t == 0) & (h == 0))
    def _():
        s0, s1, s2, s3 = tie_ref[0], tie_ref[1], tie_ref[2], tie_ref[3]
        fetch.start()
        square_ref[...] = jnp.zeros_like(square_ref)
        gain = gains_ref.shape[-1]
        square_ref[0:1, :gain] = gains_ref[s0].astype(F32)[0:1]
        square_ref[1:2, :gain] = gains_ref[s2].astype(F32)[1:2]
        kinds = [s0, s0, s0, s1, s2, s3, s2, s2, s2, s2]
        for i, source in enumerate(kinds):
            wide = bias_ref[i].astype(F32)
            here = lax.broadcasted_iota(jnp.int32, wide.shape, 0) == source
            square_ref[2 + i : 3 + i, :gain] = jnp.sum(
                jnp.where(here, wide, 0.0), 0, keepdims=True
            )
        vec_ref[...] = square_ref[...].T[:gain]
        for j in range(3):
            own0_ref[:, j * width : (j + 1) * width] = in_ref[s0, j]
        own0_ref[:, 3 * width :] = out_ref[s1].T
        place.greet(place.same_t + place.same_dp)
        start(vec_one)
        for part in halves:
            start(part.z[1], part.z[0], part.first[0])
        vecs_ref[z, y, x, c] = vec_ref[...]
        ones = lax.broadcasted_iota(jnp.int32, (vt_ref.shape[1] - HEAD_DIM, n), 0) == 0
        for h in range(heads):
            vt_ref[h, HEAD_DIM:, :] = ones.astype(BF16)
        all0_ref[0, z, y] = own0_ref[...]
        own1_ref[...] = expand_ref[s2]
        own2_ref[...] = project_ref[s3]
        w1_ref[0, z, y] = own1_ref[...]
        w2_ref[0, z, y] = own2_ref[...]
        recv(vec_one)
        start(vec_two)
        for part in halves:
            relay_z(part.z)
            start(part.first[2])
        for part in halves:
            recv(part.z[0])
            start(part.first[1])
        start(seg2.z[1])
        recv(vec_two)
        start(seg2.first)
        vecs = vecs_ref[...].reshape(D, vecs_ref.shape[-1]).T[:16]
        rows_ref[...] = vecs
        for part in halves:
            recv(part.z[2])
            start(part.first[3])
        start(seg1.first, seg0.second[0], seg0.core[0])
        for k in range(4):
            part = slice(k * width, (k + 1) * width)
            bqv_ref[k, 0:1, :width] = vecs[3:4, part]
            bqv_ref[k, 0:1, width : 2 * width] = jnp.zeros((1, width), F32)
            bqv_ref[k, 0:1, 2 * width :] = vecs[4:5, part]
        fetch.wait()

        @pl.loop(0, n // step)
        def _(b):
            rows = pl.ds(pl.multiple_of(b * step, step), step)
            wide = x_ref[rows, :].astype(F32)
            xhat, _ = norm_parts(wide)
            a1 = (xhat * rows_ref[0:1, :] + rows_ref[2:3, :]).astype(BF16)
            a1_ref[rows, :] = a1
            a1t_ref[:, rows] = a1.T
            h1_ref[rows, :] = wide + rows_ref[5:6, :]

        put_a1t.start()
        start(seg2.z[0], seg1.z[1], seg1.z[0])
        recv(halves[0].first, halves[1].first)
        start(seg0.second[1], seg0.core[1])

    serve([0])

    @pl.when(h == 0)
    def _():
        here = all0_ref[t].reshape(D, 4 * width)
        gq = here[:, : 3 * width]
        gq_ref[0] = gq
        gw_ref[0] = here[:, 3 * width :]
        mine = place.group(t)
        qkv = dot_nn(a1_ref[...], gq) + bqv_ref[mine, 0:1, :]
        q = qkv[:, :width].astype(BF16) * jnp.asarray(HEAD_DIM ** -0.5, BF16)
        k = qkv[:, width : 2 * width].astype(BF16)
        v = qkv[:, 2 * width :].astype(BF16)
        q_ref[0] = q
        kt_ref[0] = k.T
        v_ref[0] = v
        vt = v.T
        for h in range(heads):
            vt_ref[h, :HEAD_DIM, :] = vt[h * HEAD_DIM : (h + 1) * HEAD_DIM]
        spare = k_ref.shape[1] - width
        dead = lax.broadcasted_iota(jnp.int32, (n, spare), 0) >= length
        first_column = lax.broadcasted_iota(jnp.int32, (n, spare), 1) == 0
        k_ref[:, :width] = k
        k_ref[:, width:] = jnp.where(first_column & dead, MASKED, 0.0).astype(BF16)
        qa_ref[:, :width] = q
        qa_ref[:, width:] = jnp.where(first_column, 1.0, 0.0).astype(BF16)
        scale_ref[0, heads:, :] = jnp.zeros((scale_ref.shape[1] - heads, n), F32)

    serve([1])

    lane = lax.broadcasted_iota(jnp.int32, (1, qa_ref.shape[1]), 1)
    keep = ((lane >= h * HEAD_DIM) & (lane < (h + 1) * HEAD_DIM)) | (lane >= width)
    key = lax.broadcasted_iota(jnp.int32, (step, step), 0)
    query = lax.broadcasted_iota(jnp.int32, (step, step), 1)
    head = pl.ds(pl.multiple_of(h * HEAD_DIM, HEAD_DIM), HEAD_DIM)

    def scores(b):
        first, last = b * step, (b + 1) * step
        q = jnp.where(keep, qa_ref[first:last, :], jnp.zeros((), BF16))
        return dot_nt(k_ref[:last, :], q)

    def attend(b, s):
        first, last = b * step, (b + 1) * step
        near = jnp.where(key <= query, s[first:], MASKED)
        top = jnp.max(near, 0, keepdims=True)
        if b:
            far = s[:first]
            top = jnp.maximum(top, jnp.max(far, 0, keepdims=True))
        e_near = jnp.exp((near - top).astype(BF16))
        p_ref[0, 0, b, first:last, :] = e_near
        o = dot_nn(vt_ref[h, :, first:last], e_near)
        if b:
            e_far = jnp.exp((far - top).astype(BF16))
            p_ref[0, 0, b, :first, :] = e_far
            o += dot_nn(vt_ref[h, :, :first], e_far)
        scale = 1.0 / o[HEAD_DIM : HEAD_DIM + 1]
        scale_ref[0, pl.ds(h, 1), first:last] = scale
        ot_ref[head, first:last] = (o[:HEAD_DIM] * scale).astype(BF16)

    s = scores(0)
    for b in range(n // step):
        ahead = scores(b + 1) if b + 1 < n // step else None
        attend(b, s)
        s = ahead

    serve([2, 3, 4])

    @pl.when(h == heads - 1)
    def _():
        o = ot_ref[...].T
        o_ref[0] = o
        h1_ref[...] += dot_nt(o, gw_ref[0])

    @pl.when((t == 3) & (h == heads - 1))
    def _():
        for i, rows in enumerate(blocks(n, step)):
            xhat, _ = norm_parts(h1_ref[rows, :])
            a2 = (xhat * rows_ref[1:2, :] + rows_ref[6:7, :]).astype(BF16)
            a2_ref[rows, :] = a2
            a2t_ref[:, rows] = a2.T
            for put in puts[i]:
                put.start()
        put_a2t.start()
        recv(seg2.core)
        flush[1][1].start()
        recv(seg1.core)
        flush[0][1].start()
        pass_second(seg1)
        flush[0][2].start()
        links.sent()
        for copies in flush + puts + [[put_a1t, put_a2t]]:
            for copy in copies:
                copy.wait()


N_GATHER = 10 + 14 + 6 + 10 + 10
VMEM_WHOLE = pl.BlockSpec(memory_space=pltpu.VMEM)
ANY_WHOLE = pl.BlockSpec(memory_space=pl.ANY)


def run_fused_forward(tie, lengths, tokens, gains, biases, w_in, w_out, w_expand, w_project):
    groups, n, _ = tokens.shape
    depth, width = w_in.shape[-2:]
    heads = width // HEAD_DIM
    hidden = w_expand.shape[-1]
    w_project = w_project.transpose(0, 2, 1)
    biases = biases.transpose(1, 0, 2)
    own = gains.shape[-1]

    def group(*shape):
        return pl.BlockSpec((1,) + shape, lambda t, h: (t,) + (0,) * len(shape))

    per_head = pl.BlockSpec((1, 1, n // 256, n, 256), lambda t, h: (t, h, 0, 0, 0))
    return pl.pallas_call(
        fused_forward,
        grid=(groups, heads),
        in_specs=[SMEM_WHOLE, SMEM_WHOLE, ANY_WHOLE] + [VMEM_WHOLE] * 6,
        out_specs=[
            group(D, 3 * width), group(D, width), ANY_WHOLE, ANY_WHOLE, VMEM_WHOLE,
            group(n, width), group(n, width), group(width, n), per_head,
            group(8, n), group(n, width), ANY_WHOLE, ANY_WHOLE, ANY_WHOLE, ANY_WHOLE,
        ],
        out_shape=[
            shaped(BF16, groups, D, 3 * width), shaped(BF16, groups, D, width),
            shaped(BF16, groups, Z_DEV, Y_DEV, depth, hidden),
            shaped(BF16, groups, Z_DEV, Y_DEV, depth, hidden),
            shaped(F32, 16, D),
            shaped(BF16, groups, n, width), shaped(BF16, groups, n, width),
            shaped(BF16, groups, width, n), shaped(BF16, groups, heads, n // 256, n, 256),
            shaped(F32, groups, 8, n), shaped(BF16, groups, n, width), shaped(BF16, D, n), shaped(F32, n, D),
            shaped(BF16, n, D), shaped(BF16, D, n),
        ],
        scratch_shapes=[
            pltpu.VMEM((depth, 4 * width), BF16),
            pltpu.VMEM((depth, hidden), BF16), pltpu.VMEM((depth, hidden), BF16),
            pltpu.VMEM((128, 128), F32), pltpu.VMEM((own, 128), F32),
            pltpu.VMEM((groups, Z_DEV, Y_DEV, depth, 4 * width), BF16),
            pltpu.VMEM((groups, Z_DEV, Y_DEV, depth, hidden), BF16),
            pltpu.VMEM((groups, Z_DEV, Y_DEV, depth, hidden), BF16),
            pltpu.VMEM((Z_DEV, Y_DEV, X_DEV, C_DEV, own, 128), F32),
            pltpu.VMEM((groups, 8, 3 * width), F32),
            pltpu.VMEM((n, D), BF16), pltpu.VMEM((n, D), BF16), pltpu.VMEM((n, 256), BF16),
            pltpu.VMEM((n, 256), BF16), pltpu.VMEM((heads, HEAD_DIM + 16, n), BF16),
            pltpu.VMEM((width, n), BF16),
            pltpu.VMEM((D, n), BF16), pltpu.VMEM((n, D), F32), pltpu.VMEM((n, D), BF16),
            pltpu.VMEM((D, n), BF16),
            pltpu.SemaphoreType.DMA((N_GATHER,)), pltpu.SemaphoreType.DMA((N_GATHER,)),
            pltpu.SemaphoreType.DMA((3,)), pltpu.SemaphoreType.DMA((2, 4)),
            pltpu.SemaphoreType.DMA((2, n // 256)),
        ],
        compiler_params=pltpu.CompilerParams(
            vmem_limit_bytes=VMEM_LIMIT, collective_id=0, has_side_effects=True
        ),
        name="fused_forward",
    )(tie, lengths, tokens, gains, biases, w_in, w_out, w_expand, w_project)


class Result:
    def __init__(self, links, place, own_ref, passing_ref, out_ref, step, sem, count, first_ref=None):
        self.x, self.core, self.far, self.keep, self.keep_far = [], [], [], [], []
        for i in range(count):
            rows = pl.ds(i * step, step)
            mine, theirs = out_ref.at[place.t, rows], out_ref.at[place.ts[2], rows]
            own, passing = own_ref.at[rows], passing_ref.at[rows]
            source = own if first_ref is None else first_ref.at[rows]
            self.x.append(links.add(place.to_x, source, passing))
            self.core.append(links.add(place.to_core, own, mine))
            self.far.append(links.add(place.to_core, passing, theirs))
            self.keep.append(pltpu.make_async_copy(own, mine, sem.at[0, i]))
            self.keep_far.append(pltpu.make_async_copy(passing, theirs, sem.at[1, i]))

    def send(self, i):
        start(self.x[i], self.core[i], self.keep[i])

    def pass_on(self, i):
        recv(self.x[i])
        start(self.far[i], self.keep_far[i])

    def finish(self):
        recv(self.core, self.far)
        for copy in self.keep + self.keep_far:
            copy.wait()


def low(value):
    return jnp.asarray(value, BF16)


def pair_order(i):
    return i + 1 - 2 * (i % 2)


def fused_feed_forward(
    len_ref, cot_ref, a2_ref, a2t_in, h1_in, far1_ref, far2_ref, rows_ref,
    out_out, fold_ref, work_out, dh1_out, gb_out, gbt_out, sums_ref,
    gf_ref, gft_ref, feed_ref, da2_ref, h_ref, df_ref, weights_ref, missing_ref, third_ref,
    stage_ref, land_ref, near_ref, cross_ref, a2t_ref, h1_ref, out_ref, work_ref,
    send_sem, recv_sem, local_sem, row_sem,
):
    t = pl.program_id(0)
    n = gf_ref.shape[0]
    step = 256
    depth = stage_ref.shape[-2]
    place = Place()
    length = len_ref[place.t]
    links = Links(send_sem, recv_sem)
    y, other = place.y, place.other_y
    last = [
        links.add(place.to_x, far1_ref.at[0, :, other], missing_ref.at[0, 0]),
        links.add(place.to_y, far2_ref.at[2, :, y], missing_ref.at[1, 0]),
    ]
    last_core = [
        links.add(place.to_core, missing_ref.at[i, 0], missing_ref.at[i, 1]) for i in range(2)
    ]
    third = [
        links.add(place.to_core, far_ref.at[2, :, y], third_ref.at[i])
        for i, far_ref in enumerate([far1_ref, far2_ref])
    ]
    core = [
        [links.add(place.to_core, stage_ref.at[i], land_ref.at[s, i]) for i in range(2)]
        for s in range(2)
    ]
    cross = [
        links.add(place.to_y, near_ref.at[i, :, other], cross_ref.at[i]) for i in range(2)
    ]
    fetch = pltpu.make_async_copy(cot_ref.at[place.t], gf_ref, local_sem.at[0])
    gb_ref, gbt_ref, dh1_ref = gf_ref, gft_ref, da2_ref
    late = [
        pltpu.make_async_copy(a2t_in, a2t_ref, local_sem.at[5]),
        pltpu.make_async_copy(h1_in, h1_ref, local_sem.at[6]),
    ]
    puts = []
    for i in range(n // step):
        rows = pl.ds(i * step, step)
        puts.append([
            pltpu.make_async_copy(ref.at[rows], out.at[rows], row_sem.at[j, i])
            for j, (ref, out) in enumerate(
                [(out_ref, out_out), (dh1_ref, dh1_out), (gb_ref, gb_out)]
            )
        ])
    put_gbt = pltpu.make_async_copy(gbt_ref, gbt_out, local_sem.at[7])
    put_work = pltpu.make_async_copy(work_ref, work_out, local_sem.at[8])
    k = pair_order(t)
    mine = place.group(k)

    def load(step, whole, slot):
        for i, far_ref in enumerate([far1_ref, far2_ref]):
            group = far_ref.at[pair_order(step)]
            to = weights_ref.at[slot, i]
            if not whole:
                group, to = group.at[:, y], to.at[:, y]
            yield pltpu.make_async_copy(group, to, local_sem.at[1 + 2 * slot + i])

    def live_rows(b):
        at = b * step + lax.broadcasted_iota(jnp.int32, (step, 1), 0)
        return (at < length).astype(F32)

    @pl.when(t == 0)
    def _():
        fetch.start()
        for copy in load(0, True, 0):
            copy.start()
        for copy in late:
            copy.start()
        place.greet()
        start(last, third)
        sums_ref[...] = jnp.zeros_like(sums_ref)
        feed_ref[...] = jnp.zeros_like(feed_ref)
        da2_ref[...] = jnp.zeros_like(da2_ref)
        fetch.wait()

        @pl.loop(0, n // step)
        def _(b):
            rows = pl.ds(pl.multiple_of(b * step, step), step)
            g = (gf_ref[rows, :].astype(F32) * live_rows(b)).astype(BF16)
            gf_ref[rows, :] = g
            gft_ref[:, rows] = g.T
            sums_ref[7:8, :] += jnp.sum(g.astype(F32), 0, keepdims=True)

    for i in range(4):
        @pl.when(t == i)
        def _():
            if i == 2:
                recv(last_core, third)
            else:
                for copy in load(i, i < 2, i % 2):
                    copy.wait()
            if i in (0, 2):
                for copy in load(i + 1, i + 1 < 2, (i + 1) % 2):
                    copy.start()
            for j in range(2):
                if i == 2:
                    weights_ref[0, j, :, y] = third_ref[j]
                if i >= 2:
                    weights_ref[i % 2, j, :, other] = missing_ref[j, 3 - i]

    bias = rows_ref[pl.ds(8 + mine, 1), :]
    w1 = weights_ref[t % 2, 0].reshape(D, -1)
    w2 = weights_ref[t % 2, 1].reshape(D, -1)
    column = jnp.zeros((1, w1.shape[1]), F32)
    for rows in blocks(n, step):
        f = (dot_nn(a2_ref[rows, :], w1) + bias).astype(BF16)
        dh = dot_nn(gf_ref[rows, :], w2)
        f2 = f * f
        th = jnp.tanh(f * (low(SQRT_2_PI) + low(SQRT_2_PI * 0.044715) * f2))
        half = low(0.5) + low(0.5) * th
        h = f * half
        slope = half + f * (low(0.5) - low(0.5) * th * th) * (
            low(SQRT_2_PI) + low(3 * SQRT_2_PI * 0.044715) * f2
        )
        df = (dh * slope.astype(F32)).astype(BF16)
        h_ref[rows, :] = h
        df_ref[rows, :] = df
        column += jnp.sum(df.astype(F32), 0, keepdims=True)
        feed_ref[rows, :] += dot_nt(h, w2)
        da2_ref[rows, :] += dot_nt(df, w1)
    sums_ref[pl.ds(8 + mine, 1), :] = column

    @pl.when(t == 1)
    def _():
        recv(last)
        start(last_core)

    @pl.when(t == 0)
    def _():
        late[0].wait()

    def weight_grad(left_ref, right_ref):
        value = dot_nn(left_ref[...], right_ref[...])
        return value.reshape(Z_DEV, Y_DEV, depth, value.shape[-1]).astype(BF16)

    grad1 = weight_grad(a2t_ref, df_ref)
    grad2 = weight_grad(gft_ref, h_ref)

    def put(ref):
        ref[0] = grad1
        ref[1] = grad2

    def reduced(ref):
        return lambda i, s, z: (
            ref[i, z].astype(F32) + land_ref[s, i, z].astype(F32)
        ).astype(BF16)

    @pl.when(t == 0)
    def _():
        put(stage_ref)
        start(core[0])

    @pl.when(t == 1)
    def _():
        put(near_ref)
        recv(core[0])

        @pl.loop(0, Z_DEV)
        def _(z):
            for i in range(2):
                near_ref[i, z] = reduced(near_ref)(i, 0, z)

        start(cross)

    @pl.when(t == 2)
    def _():
        for copy in core[0]:
            copy.wait_send()
        put(stage_ref)
        start(core[1])

    @pl.when(t == 3)
    def _():
        put(work_ref)
        late[1].wait()
        for i, rows in enumerate(blocks(n, step)):
            live = live_rows(i)
            h1 = h1_ref[rows, :]
            out_ref[rows, :] = (live * (h1 + (feed_ref[rows, :] + rows_ref[7:8, :]))).astype(BF16)
            xhat, r = norm_parts(h1)
            da2 = da2_ref[rows, :]
            sums_ref[1:2, :] += jnp.sum(da2 * xhat, 0, keepdims=True)
            sums_ref[6:7, :] += jnp.sum(da2, 0, keepdims=True)
            dg = da2 * rows_ref[1:2, :]
            dv = r * (
                dg
                - jnp.mean(dg, -1, keepdims=True)
                - xhat * jnp.mean(dg * xhat, -1, keepdims=True)
            )
            dh1 = gf_ref[rows, :].astype(F32) + dv
            dh1_ref[rows, :] = dh1
            gb = dh1.astype(BF16)
            gb_ref[rows, :] = gb
            gbt_ref[:, rows] = gb.T
            sums_ref[5:6, :] += jnp.sum(gb.astype(F32), 0, keepdims=True)
            for copy in puts[i]:
                copy.start()
        put_gbt.start()
        recv(core[1])

        @pl.loop(0, Z_DEV)
        def _(z):
            for i in range(2):
                work_ref[i, z] = reduced(work_ref)(i, 1, z)

        put_work.start()
        recv(cross)

        @pl.loop(0, Z_DEV)
        def _(z):
            for i in range(2):
                fold_ref[i, z] = (
                    near_ref[i, z, y].astype(F32) + cross_ref[i, z].astype(F32)
                ).astype(BF16)

        links.sent(*core[0])
        for copies in puts + [[put_gbt, put_work]]:
            for copy in copies:
                copy.wait()


def run_fused_feed_forward(lengths, cot, a2, a2t, h1, g1, g2, rows):
    n = cot.shape[1]
    groups, _, _, depth, hidden = g1.shape
    both = (2, Z_DEV, Y_DEV, depth, hidden)
    fold = (2, Z_DEV, depth, hidden)
    return pl.pallas_call(
        fused_feed_forward,
        grid=(groups,),
        in_specs=[SMEM_WHOLE, ANY_WHOLE, VMEM_WHOLE] + [ANY_WHOLE] * 4 + [VMEM_WHOLE],
        out_specs=[ANY_WHOLE, VMEM_WHOLE] + [ANY_WHOLE] * 4 + [VMEM_WHOLE],
        out_shape=[
            shaped(BF16, n, D), shaped(BF16, *fold), shaped(BF16, *both), shaped(F32, n, D),
            shaped(BF16, n, D), shaped(BF16, D, n), shaped(F32, 16, D),
        ],
        scratch_shapes=[
            pltpu.VMEM((n, D), BF16), pltpu.VMEM((D, n), BF16), pltpu.VMEM((n, D), F32),
            pltpu.VMEM((n, D), F32), pltpu.VMEM((n, hidden), BF16), pltpu.VMEM((n, hidden), BF16),
            pltpu.VMEM((2,) + both, BF16),
            pltpu.VMEM((2,) + fold, BF16), pltpu.VMEM(fold, BF16), pltpu.VMEM(both, BF16),
            pltpu.VMEM((2,) + both, BF16),
            pltpu.VMEM(both, BF16), pltpu.VMEM(fold, BF16),
            pltpu.VMEM((D, n), BF16), pltpu.VMEM((n, D), F32), pltpu.VMEM((n, D), BF16),
            pltpu.VMEM(both, BF16),
            pltpu.SemaphoreType.DMA((12,)), pltpu.SemaphoreType.DMA((12,)),
            pltpu.SemaphoreType.DMA((9,)), pltpu.SemaphoreType.DMA((3, n // 256)),
        ],
        compiler_params=pltpu.CompilerParams(
            vmem_limit_bytes=VMEM_LIMIT, collective_id=1, has_side_effects=True
        ),
        name="fused_feed_forward",
    )(lengths, cot, a2, a2t, h1, g1, g2, rows)
class Reduce:
    def __init__(
        self, links, place, work, acc, cross_ref, far_ref, mid_ref, last_ref, side_ref,
        slots=(0, 1),
    ):
        self.place, self.work, self.acc = place, work, acc
        self.cross_ref, self.far_ref, self.mid_ref = cross_ref, far_ref, mid_ref
        self.last_ref, self.side_ref = last_ref, side_ref
        self.two = len(slots) == 2
        zs = place.zs
        self.y = {
            s: [
                links.add(
                    place.to_y, work(s, zs[j], place.other_y),
                    cross_ref.at[s if self.two else 0, zs[j]],
                )
                for j in (1, 3, 2, 0)
            ]
            for s in slots
        }
        self.z = [
            [
                links.add(place.to_z[1], acc(s, zs[1]), far_ref.at[s, 0]),
                links.add(place.to_z[1], acc(s, zs[3]), far_ref.at[s, 1]),
                links.add(place.to_z[2], mid_ref.at[s, 1], far_ref.at[s, 2]),
            ]
            for s in range(2)
        ]
        self.x = links.add(place.to_x, last_ref, side_ref)

    def fold_y(self, s, half):
        for i, j in [(0, 1), (1, 3), (2, 2), (3, 0)][2 * half : 2 * half + 2]:
            z = self.place.zs[j]
            recv(self.y[s][i])
            value = self.work(s, z, self.place.y)[...].astype(F32)
            cross = self.cross_ref[s if self.two else 0, z].astype(F32)
            self.acc(s, z)[...] = (value + cross).astype(BF16)
            if i < 2:
                start(self.z[s][i])

    def fold_z(self, s):
        recv(self.z[s][:2])
        for i in (1, 0):
            value = self.acc(s, self.place.zs[2 * i])[...].astype(F32)
            self.mid_ref[s, i] = (value + self.far_ref[s, i].astype(F32)).astype(BF16)
            if i:
                start(self.z[s][2])

    def own(self, s):
        recv(self.z[s][2])
        return self.mid_ref[s, 0].astype(F32) + self.far_ref[s, 2].astype(F32)

    def send_x(self):
        self.last_ref[...] = self.own(1).astype(BF16)
        start(self.x)

    def total(self):
        value = self.own(0)
        recv(self.x)
        return value + self.side_ref[...].astype(F32)


def fused_backward(
    tokens_ref, gq_in, gw_in, rows_ref, dh1_ref, gb_ref, gbt_in, q_in, v_in, kt_in,
    p_ref, scale_in, o_in, a1t_in, layer_in, fold_in, work_in, early_ref,
    out_ref, layerout_ref, part0_ref, part1_ref, part2_ref, total_ref,
    gq_ref, gw_ref, q_ref, v_ref, kt_ref, scale_ref, o_ref,
    a1t_ref, gbt_ref, layer_ref, fold_ref, work_ref, do_ref, delta_ref, dkv_ref, dqkv_ref, hold_ref, da1_ref, own_ref, passing_ref, passlayer_ref, bqv_ref,
    folded_ref, cross1_ref, far1_ref, mid1_ref, last1_ref, side1_ref,
    cross2_ref, far2_ref, mid2_ref, last2_ref, side2_ref,
    stage0_ref, land0_ref, work0_ref, cross0_ref, far0_ref, mid0_ref, last0_ref, side0_ref,
    sums_ref, sumland_ref,
    send_sem, recv_sem, local_sem, result_sem, group_sem,
):
    t = pl.program_id(0)
    n = own_ref.shape[0]
    width = gw_ref.shape[-1]
    depth = part0_ref.shape[0]
    heads = width // HEAD_DIM
    step = n // 4
    place = Place()
    y = place.y
    links = Links(send_sem, recv_sem)
    k, i = group_and_block(t)
    mine = place.group(k)
    now = k % 2
    out = Result(links, place, own_ref, passing_ref, out_ref, step, result_sem.at[0], 4)
    layer = Result(
        links, place, layer_ref, passlayer_ref, layerout_ref, step, result_sem.at[1], 4, layer_in
    )
    fetch = pltpu.make_async_copy(tokens_ref.at[place.t], own_ref, local_sem.at[0])
    fetch_layer, fetch_work, fetch_fold, fetch_gbt, fetch_a1t = [
        pltpu.make_async_copy(there, here, local_sem.at[1 + j])
        for j, (there, here) in enumerate([
            (layer_in, layer_ref), (work_in, work_ref), (fold_in, fold_ref),
            (gbt_in, gbt_ref), (a1t_in, a1t_ref),
        ])
    ]
    def operands(group):
        slot = group % 2
        pairs = [
            (gw_in, gw_ref), (scale_in, scale_ref), (o_in, o_ref), (v_in, v_ref),
            (q_in, q_ref), (kt_in, kt_ref), (gq_in, gq_ref),
        ]
        return [
            pltpu.make_async_copy(there.at[group], here.at[slot], group_sem.at[slot, j])
            for j, (there, here) in enumerate(pairs)
        ]

    core0 = [links.add(place.to_core, stage0_ref, land0_ref.at[i]) for i in range(2)]
    def half_done(i, *landing):
        return Reduce(
            links, place, lambda s, z, y: work_ref.at[i, z, y],
            lambda s, z: folded_ref.at[i, z] if s else fold_ref.at[i, z],
            *landing, slots=(1,),
        )

    seg1 = half_done(0, cross1_ref, far1_ref, mid1_ref, last1_ref, side1_ref)
    seg2 = half_done(1, cross2_ref, far2_ref, mid2_ref, last2_ref, side2_ref)
    seg0 = Reduce(
        links, place, lambda s, z, y: work0_ref.at[s, z, y],
        lambda s, z: work0_ref.at[s, z, y],
        cross0_ref, far0_ref, mid0_ref, last0_ref, side0_ref,
    )
    sum_core, sum_y, *sum_z, sum_x = [
        links.add(to, sums_ref.at[i], sumland_ref.at[j])
        for j, (i, to) in enumerate(
            zip([0, 1, 2, 2, 2, 3], [place.to_core, place.to_y] + place.to_z[1:] + [place.to_x])
        )
    ]

    def when(point):
        return pl.when(t == point)

    @when(0)
    def _():
        start(fetch_layer, operands(1), fetch_work, fetch_fold, fetch_gbt, operands(0))
        start(fetch, fetch_a1t)
        place.greet()
        @pl.when(place.c == 0)
        def _():
            start(layer.x)

        fetch_work.wait()
        start(seg1.y[1], seg2.y[1])
        fetch_fold.wait()
        start(seg1.z[0][:2], seg2.z[0][:2])

        @pl.when(place.c == 1)
        def _():
            start(layer.x)

        fetch_layer.wait()
        start(layer.core, layer.keep)
        bqv_ref[...] = jnp.zeros_like(bqv_ref)
        sums_ref[0] = early_ref[...]
        fetch_gbt.wait()

    def wait(copies):
        for copy in copies:
            copy.wait()

    @when(0)
    def _():
        wait(operands(1))

    @when(4)
    def _():
        start(operands(3))
        wait(operands(0))

    @when(8)
    def _():
        start(operands(2))
        wait(operands(3))

    @when(9)
    def _():
        wait(operands(2))

    plan = [
        (2, 1, lambda: (seg1.fold_y(1, 0), seg1.fold_z(0))),
        (3, 1, lambda: layer.pass_on(0)),
        (4, 0, lambda: (seg1.fold_y(1, 1), seg2.fold_z(0))),
        (4, 1, lambda: layer.pass_on(1)),
        (5, 1, lambda: (seg1.fold_z(1), seg2.fold_y(1, 0))),
        (8, 0, lambda: (seg2.fold_y(1, 1), layer.pass_on(2))),
        (8, 1, lambda: seg1.send_x()),
        (9, 1, lambda: (seg2.fold_z(1), seg0.fold_y(0, 0), layer.pass_on(3))),
        (11, 1, lambda: (seg2.send_x(), seg0.fold_y(0, 1))),
        (13, 1, lambda: (seg0.fold_z(0), out.pass_on(3))),
    ]

    def serve(point):
        for at, where, act in plan:
            if where == point:
                pl.when(t == at)(lambda act=act: (act(), None)[1])

    @pl.when((t == 0) | (t == 4) | (t == 8) | (t == 9))
    def _():
        pick = (
            lax.broadcasted_iota(jnp.int32, (8, width), 1) // HEAD_DIM
            == lax.broadcasted_iota(jnp.int32, (8, width), 0)
        ).astype(BF16)

        @pl.loop(0, n // step)
        def _(i):
            rows = pl.ds(pl.multiple_of(i * step, step), step)
            columns = scale_ref[now, :, rows].T
            lane = lax.broadcasted_iota(jnp.int32, (step, width), 1)
            scale = columns[:, heads - 1 : heads]
            for h in reversed(range(heads - 1)):
                scale = jnp.where(lane < (h + 1) * HEAD_DIM, columns[:, h : h + 1], scale)
            do = (dot_nn(gb_ref[rows, :], gw_ref[now]) * scale).astype(BF16)
            do_ref[now, rows, :] = do
            product = do.astype(F32) * o_ref[now, rows, :].astype(F32)
            high = product.astype(BF16)
            low = (product - high.astype(F32)).astype(BF16)
            delta_ref[now, :, rows] = dot_nt(pick, high) + dot_nt(pick, low)

        value = dot_nn(gbt_ref[...], o_ref[now]).astype(BF16)
        value = value.reshape(Z_DEV, Y_DEV, depth, width)

        hold_ref[now] = value

    serve(0)

    for ii in reversed(range(4)):
        @pl.when(i == ii)
        def _():
            first, last = ii * step, (ii + 1) * step
            do = do_ref[now, first:last, :]
            q = q_ref[now, first:last, :]
            v = v_ref[now, :last, :]
            lane = lax.broadcasted_iota(jnp.int32, (1, width), 1)
            dk, dv, dq = None, None, []
            for h in range(heads):
                low, high = h * HEAD_DIM, (h + 1) * HEAD_DIM
                here = (lane >= low) & (lane < high)
                p = p_ref[0, h, 0, :last, :]
                dp = dot_nt(v, jnp.where(here, do, jnp.zeros((), BF16)))
                ds = p * (dp - delta_ref[now, h : h + 1, first:last]).astype(BF16)
                part = dot_nn(p, do)
                dv = part if dv is None else jnp.where(lane < low, dv, part)
                part = dot_nn(ds, q)
                dk = part if dk is None else jnp.where(lane < low, dk, part)
                dq.append(dot_nn(kt_ref[now, low:high, :last], ds))
            if ii == 3:
                dkv_ref[now, 0] = dk
                dkv_ref[now, 1] = dv
            else:
                dkv_ref[now, 0, :last, :] += dk
                dkv_ref[now, 1, :last, :] += dv
            dk = dkv_ref[now, 0, first:last, :].astype(BF16)
            dv = dkv_ref[now, 1, first:last, :].astype(BF16)
            dq = (jnp.concatenate(dq, 0) * HEAD_DIM ** -0.5).astype(BF16).T
            dqkv_ref[now, first:last, :width] = dq
            dqkv_ref[now, first:last, width : 2 * width] = dk
            dqkv_ref[now, first:last, 2 * width :] = dv
            bqv_ref[mine, 0:1, :] += jnp.sum(dq.astype(F32), 0, keepdims=True)
            bqv_ref[mine, 1:2, :] += jnp.sum(dv.astype(F32), 0, keepdims=True)

            @pl.when(t >= 8)
            def _():
                da1_ref[first:last, :] += dot_nt(dqkv_ref[now, first:last, :], gq_ref[now])

    serve(1)

    @pl.when((t == 3) | (t == 7) | (t > 13))
    def _():
        @when(3)
        def _():
            fetch.wait()
            fetch_a1t.wait()

        @when(3)
        def _():
            da1_ref[...] = dot_nt(dqkv_ref[now], gq_ref[now])

        @when(7)
        def _():
            da1_ref[...] += dot_nt(dqkv_ref[now], gq_ref[now])

        value = dot_nn(a1t_ref[...], dqkv_ref[now]).reshape(Z_DEV, Y_DEV, depth, 3 * width)
        value = jnp.concatenate([value, hold_ref[now].astype(F32)], -1)
        for s in range(2):
            @when(3 + 11 * s)
            def _():
                if s:
                    core0[0].wait_send()
                stage0_ref[...] = value.astype(BF16)
                start(core0[s])

            @when(7 + 8 * s)
            def _():
                recv(core0[s])
                work0_ref[s] = (value + land0_ref[s].astype(F32)).astype(BF16)
                start(seg0.y[s])

    @pl.when((t > 8) & (t % 2 == 1))
    def _():
        rows = pl.ds(pl.multiple_of(i * step, step), step)
        xhat, r = norm_parts(own_ref[rows, :].astype(F32))
        da1 = da1_ref[rows, :]
        sums_ref[0, 0:1, :] += jnp.sum(da1 * xhat, 0, keepdims=True)
        sums_ref[0, 2:3, :] += jnp.sum(da1, 0, keepdims=True)
        dg = da1 * rows_ref[0:1, :]
        dv = r * (
            dg
            - jnp.mean(dg, -1, keepdims=True)
            - xhat * jnp.mean(dg * xhat, -1, keepdims=True)
        )
        own_ref[rows, :] = (dh1_ref[...] + dv).astype(BF16)
        for ii in range(4):
            @pl.when(i == ii)
            def _():
                out.send(ii)

    @when(15)
    def _():
        for s in range(4):
            sums_ref[0, 3:5, s * width : (s + 1) * width] = bqv_ref[s, 0:2, :]
        start(sum_core)
        out.pass_on(2)
        recv(sum_core)
        sums_ref[1] = sums_ref[0] + sumland_ref[0]
        start(sum_y)
        seg0.fold_y(1, 0)
        out.pass_on(1)
        seg0.fold_y(1, 1)
        recv(sum_y)
        sums_ref[2] = sums_ref[1] + sumland_ref[1]
        start(sum_z)
        seg0.fold_z(1)
        recv(sum_z)
        sums_ref[3] = (sums_ref[2] + sumland_ref[2]) + (sumland_ref[3] + sumland_ref[4])
        start(sum_x)
        part1_ref[...] = seg1.total()
        part2_ref[...] = seg2.total()
        seg0.send_x()
        layer.finish()
        out.pass_on(0)
        recv(sum_x)
        total_ref[...] = sums_ref[3] + sumland_ref[5]
        part0_ref[...] = seg0.total()
        out.finish()
        links.sent(core0[0])


def group_and_block(t):
    early = t < 8
    return (
        jnp.where(early, 1 - t // 4, 3 - t % 2),
        3 - jnp.where(early, t % 4, jnp.maximum(t - 8, 0) // 2),
    )


def run_fused_backward(
    tokens, gq, gw, rows, dh1, gb, gbt, q, v, kt, p, scale, o, a1t, layer, fold, work, early
):
    groups, n, _ = tokens.shape
    width = gw.shape[-1]
    heads = width // HEAD_DIM
    hidden = fold.shape[-1]
    depth = D // (Z_DEV * Y_DEV)
    step = n // 4

    p_spec = pl.BlockSpec(
        (1, heads, 1, n, step),
        lambda t: (group_and_block(t)[0], 0, group_and_block(t)[1], 0, 0),
    )

    copies = 2 * 12 + 2 + 15 + 2 * 11 + 6

    def landing(lanes, slots=1):
        return [
            pltpu.VMEM((slots, Z_DEV, depth, lanes), BF16),
            pltpu.VMEM((2, 3, depth, lanes), BF16), pltpu.VMEM((2, 2, depth, lanes), BF16),
            pltpu.VMEM((depth, lanes), BF16), pltpu.VMEM((depth, lanes), BF16),
        ]

    def working(lanes):
        block = (Z_DEV, Y_DEV, depth, lanes)
        return [pltpu.VMEM(block, BF16)] + [pltpu.VMEM((2,) + block, BF16)] * 2

    return pl.pallas_call(
        fused_backward,
        grid=(4 * groups,),
        in_specs=[
            ANY_WHOLE, ANY_WHOLE, ANY_WHOLE, VMEM_WHOLE,
            pl.BlockSpec((step, D), lambda t: (group_and_block(jnp.maximum(t, 8))[1], 0)),
            VMEM_WHOLE, ANY_WHOLE, ANY_WHOLE, ANY_WHOLE, ANY_WHOLE, p_spec,
            ANY_WHOLE, ANY_WHOLE, ANY_WHOLE, ANY_WHOLE, ANY_WHOLE, ANY_WHOLE, VMEM_WHOLE,
        ],
        out_specs=[ANY_WHOLE] * 2 + [VMEM_WHOLE] * 4,
        out_shape=[
            shaped(BF16, groups, n, D), shaped(BF16, groups, n, D),
            shaped(F32, depth, 4 * width), shaped(F32, depth, hidden),
            shaped(F32, depth, hidden), shaped(F32, 16, D),
        ],
        scratch_shapes=[
            pltpu.VMEM((2, D, 3 * width), BF16), pltpu.VMEM((2, D, width), BF16),
            pltpu.VMEM((2, n, width), BF16), pltpu.VMEM((2, n, width), BF16),
            pltpu.VMEM((2, width, n), BF16), pltpu.VMEM((2, 8, n), F32),
            pltpu.VMEM((2, n, width), BF16),
            pltpu.VMEM((D, n), BF16), pltpu.VMEM((D, n), BF16), pltpu.VMEM((n, D), BF16),
            pltpu.VMEM((2, Z_DEV, depth, hidden), BF16),
            pltpu.VMEM((2, Z_DEV, Y_DEV, depth, hidden), BF16),
            pltpu.VMEM((2, n, width), BF16),
            pltpu.VMEM((2, 8, n), F32), pltpu.VMEM((2, 2, n, width), F32),
            pltpu.VMEM((2, n, 3 * width), BF16),
            pltpu.VMEM((2, Z_DEV, Y_DEV, depth, width), BF16), pltpu.VMEM((n, D), F32),
            pltpu.VMEM((n, D), BF16), pltpu.VMEM((n, D), BF16), pltpu.VMEM((n, D), BF16),
            pltpu.VMEM((groups, 8, width), F32),
        ]
        + [pltpu.VMEM((2, Z_DEV, depth, hidden), BF16)] + landing(hidden) + landing(hidden)
        + working(4 * width) + landing(4 * width, 2)
        + [
            pltpu.VMEM((4, 16, D), F32), pltpu.VMEM((6, 16, D), F32),
            pltpu.SemaphoreType.DMA((copies,)), pltpu.SemaphoreType.DMA((copies,)),
            pltpu.SemaphoreType.DMA((6,)), pltpu.SemaphoreType.DMA((2, 2, 4)),
            pltpu.SemaphoreType.DMA((2, 7)),
        ],
        compiler_params=pltpu.CompilerParams(
            vmem_limit_bytes=VMEM_LIMIT, collective_id=2, has_side_effects=True
        ),
        name="fused_backward",
    )(tokens, gq, gw, rows, dh1, gb, gbt, q, v, kt, p, scale, o, a1t, layer, fold, work, early)


def place_gradients(
    tie_ref, sums_ref, part0_ref, part1_ref, part2_ref, near_out_ref,
    near_grad_ref, far_out_ref, far_grad_ref, gains_ref, bias_ref, in_ref, out_ref, expand_ref,
    project_ref, chosen_ref,
):
    t = pl.program_id(0)
    far_out_ref[...] = near_out_ref[...]
    far_grad_ref[...] = near_grad_ref[...]
    own = gains_ref.shape[-1]
    width = part0_ref.shape[-1] // 4
    kinds = [tie_ref[0], tie_ref[1], tie_ref[2], tie_ref[3]]

    @pl.when(t == 0)
    def _():
        first = (lax.axis_index("dp") * 4 + lax.axis_index("tensor")) * own
        feature = lax.broadcasted_iota(jnp.int32, (D, 128), 0)
        lane = lax.broadcasted_iota(jnp.int32, (D, 128), 1)
        chosen = ((feature == first + lane) & (lane < own)).astype(F32)
        chosen_ref[...] = lax.dot_general(
            sums_ref[...], chosen, (((1,), (0,)), ((), ())),
            precision=lax.Precision.HIGHEST, preferred_element_type=F32,
        )
        row = lax.broadcasted_iota(jnp.int32, (NSRC, own), 0)
        for i, kind in enumerate([0, 0, 0, 1, 2, 3, 2, 2, 2, 2]):
            value = chosen_ref[2 + i : 3 + i, :own]
            bias_ref[i] = jnp.where(row == kinds[kind], value, 0.0)

    @pl.when(t < NSRC)
    def _():
        def here(kind, value):
            return jnp.where(kinds[kind] == t, value, jnp.zeros_like(value))

        gains_ref[0, 0:1] = here(0, chosen_ref[0:1, :own])
        gains_ref[0, 1:2] = here(2, chosen_ref[1:2, :own])
        for j in range(3):
            in_ref[0, j] = here(0, part0_ref[:, j * width : (j + 1) * width])
        out_ref[0] = here(1, part0_ref[:, 3 * width :].T)
        expand_ref[0] = here(2, part1_ref[...])
        project_ref[0] = here(3, part2_ref[...])


def run_place_gradients(tie, sums, part0, part1, part2, out, grad, like):
    slots, n, _ = grad.shape
    gains, biases, w_in, w_out, w_expand, w_project = [item.shape for item in like]
    shapes = [
        gains, (biases[1], biases[0], biases[2]), w_in, w_out, w_expand,
        (w_project[0], w_project[2], w_project[1]),
    ]

    def source(shape):
        return pl.BlockSpec(
            (1,) + shape[1:], lambda t: (jnp.minimum(t, NSRC - 1),) + (0,) * (len(shape) - 1)
        )

    out, grad, gains, biases, w_in, w_out, w_expand, w_project = pl.pallas_call(
        place_gradients,
        grid=(slots,),
        in_specs=[SMEM_WHOLE] + [VMEM_WHOLE] * 4 + [group(n, D), group(n, D)],
        out_specs=[group(n, D), group(n, D), source(shapes[0]), VMEM_WHOLE]
        + [source(shape) for shape in shapes[2:]],
        out_shape=[shaped(BF16, slots, n, D)] * 2 + [shaped(F32, *item) for item in shapes],
        scratch_shapes=[pltpu.VMEM((16, 128), F32)],
        compiler_params=pltpu.CompilerParams(vmem_limit_bytes=VMEM_LIMIT),
        name="place_gradients",
    )(tie, sums, part0, part1, part2, out, grad)
    biases = biases.transpose(1, 0, 2)
    return out, grad, gains, biases, w_in, w_out, w_expand, w_project.transpose(0, 2, 1)


def plain_step(
    tokens, lengths, tie_map, norm_gains, bias_rows, attention_in, attention_out,
    expand_weight, project_weight, cotangent,
):
    slot_rows = tokens.shape[0] // lengths.shape[0]
    me = lax.axis_index("tensor")
    in_local = lax.dynamic_index_in_dim(attention_in, tie_map[0], 0, keepdims=False)
    out_local = lax.dynamic_index_in_dim(attention_out, tie_map[1], 0, keepdims=False)
    expand_local = lax.dynamic_index_in_dim(expand_weight, tie_map[2], 0, keepdims=False)
    project_local = lax.dynamic_index_in_dim(project_weight, tie_map[3], 0, keepdims=False)
    local0 = jnp.concatenate([in_local, out_local.T[None]], 0)
    row_kinds = jnp.array([0, 0, 0, 1, 2, 3] + [2] * (FF // D), dtype=jnp.int32)
    gain_kinds = jnp.array([0, 2], dtype=jnp.int32)
    gain_pick = norm_gains[tie_map[gain_kinds], jnp.arange(2)]
    bias_pick = bias_rows[tie_map[row_kinds], jnp.arange(row_kinds.shape[0])]
    vectors = jnp.concatenate([gain_pick, bias_pick], 0)
    x = lax.dynamic_slice_in_dim(tokens, me * slot_rows, slot_rows, 0)
    cot = lax.dynamic_slice_in_dim(cotangent, me * slot_rows, slot_rows, 0)
    length = lax.dynamic_slice_in_dim(lengths, me, 1, 0)
    rows = lax.all_gather(vectors, ("dp", "tensor"), axis=1, tiled=True).astype(F32)
    rows = jnp.concatenate([rows, jnp.zeros((4, D), F32)], 0)

    def gathered(piece, axis):
        piece = lax.all_gather(piece, "dp", axis=axis, tiled=True)
        return lax.all_gather(piece, "tensor", axis=0)

    g0 = gathered(local0, 1)
    g1 = gathered(expand_local, 0)
    g2 = gathered(project_local.T, 0)
    groups, width = g0.shape[0], g0.shape[-1]
    bqv = rows[3:5].reshape(2, groups, width).transpose(1, 0, 2)
    q, v, kt, p, o, a1t, h1, a2, a2t = run_attention_forward(length, x, g0, rows, bqv)
    out, d1, d2, dh1, gb, gbt, sums = run_feed_forward(length, cot, a2, a2t, h1, g1, g2, rows)
    d0, xg, sums_in, sums_qv = run_attention_backward(
        x, g0, rows, dh1, gb, gbt, q, v, kt, p, o, a1t
    )
    layer_out = lax.all_gather(out, "tensor", axis=0, tiled=True)
    tokens_grad = lax.all_gather(xg, "tensor", axis=0, tiled=True)

    def scattered(piece, axis):
        piece = lax.psum_scatter(piece, "tensor", scatter_dimension=0)
        return lax.psum_scatter(piece, "dp", scatter_dimension=axis, tiled=True).astype(F32)

    part0 = scattered(d0, 1)
    part1 = scattered(d1, 0)
    part2 = scattered(d2, 0)
    qv = sums_qv[:, :2].transpose(1, 0, 2).reshape(2, D)
    sums = jnp.concatenate(
        [sums_in[0:1], sums[1:2], sums_in[1:2], qv, sums[5:12]], 0
    )
    sums = lax.psum_scatter(sums, ("dp", "tensor"), scatter_dimension=1, tiled=True)
    return layer_out, tokens_grad, *placed(tie_map, sums, part0, part1, part2)


def fused_step(
    tokens, lengths, tie_map, norm_gains, bias_rows, attention_in, attention_out,
    expand_weight, project_weight, cotangent,
):
    slots = lengths.shape[0]
    tokens = tokens.reshape(slots, -1, D)
    cotangent = cotangent.reshape(slots, -1, D)
    gq, gw, g1, g2, rows, q, v, kt, p, scale, o, a1t, h1, a2, a2t = run_fused_forward(
        tie_map, lengths, tokens, norm_gains, bias_rows, attention_in, attention_out,
        expand_weight, project_weight,
    )
    layer, fold, work, dh1, gb, gbt, early = run_fused_feed_forward(
        lengths, cotangent, a2, a2t, h1, g1, g2, rows
    )
    grad, out, part0, part1, part2, sums = run_fused_backward(
        tokens, gq, gw, rows, dh1, gb, gbt, q, v, kt, p, scale, o, a1t, layer, fold,
        work, early,
    )
    out, grad, *placed_grads = run_place_gradients(
        tie_map, sums, part0, part1, part2, out, grad,
        (norm_gains, bias_rows, attention_in, attention_out, expand_weight, project_weight),
    )
    return out.reshape(-1, D), grad.reshape(-1, D), *placed_grads


def placed(tie_map, sums, part0, part1, part2):
    source = jnp.arange(NSRC, dtype=jnp.int32)

    def place(piece, which):
        pick = (source == tie_map[which]).reshape((NSRC,) + (1,) * piece.ndim)
        return jnp.where(pick, piece[None], 0.0)

    def place_rows(piece, kinds):
        pick = source[:, None] == tie_map[jnp.array(kinds, dtype=jnp.int32)][None, :]
        return jnp.where(pick[:, :, None], piece[None], 0.0)

    return (
        place_rows(sums[:2], [0, 2]),
        place_rows(sums[2:], [0, 0, 0, 1, 2, 3] + [2] * (FF // D)),
        place(part0[:3], 0),
        place(part0[3].T, 1),
        place(part1, 2),
        place(part2.T, 3),
    )


def solution(mesh):
    fused = mesh.shape["dp"] == Z_DEV * Y_DEV and mesh.shape["tensor"] == X_DEV * C_DEV
    return jax.shard_map(
        fused_step if fused else plain_step,
        mesh=mesh,
        in_specs=(
            P("dp", None),
            P("dp"),
            P(),
            P(None, None, ("dp", "tensor")),
            P(None, None, ("dp", "tensor")),
            P(None, None, "dp", "tensor"),
            P(None, "tensor", "dp"),
            P(None, "dp", "tensor"),
            P(None, "tensor", "dp"),
            P("dp", None),
        ),
        out_specs=(
            P("dp", None),
            P("dp", None),
            P(None, None, ("dp", "tensor")),
            P(None, None, ("dp", "tensor")),
            P(None, None, "dp", "tensor"),
            P(None, "tensor", "dp"),
            P(None, "dp", "tensor"),
            P(None, "tensor", "dp"),
        ),
        check_vma=False,
    )
```

```python
import jax
import jax.numpy as jnp
from jax import lax
from jax.experimental import pallas as pl
from jax.experimental.pallas import tpu as pltpu
from jax.sharding import PartitionSpec as P

D = 768
HEAD_DIM = 64
FF = 3072
NSRC = 4
EPS = 1e-05
MASKED = -1e30
F32 = jnp.float32
BF16 = jnp.bfloat16
VMEM_LIMIT = 60 * 1024 * 1024


def dot_nn(a, b):
    return lax.dot_general(a, b, (((1,), (0,)), ((), ())), preferred_element_type=F32)


def dot_nt(a, b):
    return lax.dot_general(a, b, (((1,), (1,)), ((), ())), preferred_element_type=F32)


def norm_parts(v):
    center = jnp.mean(v, -1, keepdims=True)
    centered = v - center
    r = lax.rsqrt(jnp.mean(centered * centered, -1, keepdims=True) + EPS)
    return centered * r, r


def head_mask(shape, h):
    lane = lax.broadcasted_iota(jnp.int32, shape, 1)
    return (lane >= h * HEAD_DIM) & (lane < (h + 1) * HEAD_DIM)


def blocks(total, size):
    return [slice(i * size, (i + 1) * size) for i in range(total // size)]


def attention_forward(
    len_ref, x_ref, g_ref, rows_ref, bqv_ref,
    q_ref, v_ref, kt_ref, p_ref, o_ref, a1t_ref, h1_ref, a2_ref, a2t_ref,
    a1_ref, k_ref, vt_ref, ot_ref, attn_ref,
):
    t = pl.program_id(0)
    n = x_ref.shape[0]
    width = g_ref.shape[-1]
    heads = width // HEAD_DIM
    step = 256
    length = len_ref[0]

    @pl.when(t == 0)
    def _():
        @pl.loop(0, n // step)
        def _(b):
            rows = pl.ds(pl.multiple_of(b * step, step), step)
            xhat, _ = norm_parts(x_ref[rows, :].astype(F32))
            a1 = xhat * rows_ref[0:1, :] + rows_ref[2:3, :]
            a1_ref[rows, :] = a1.astype(BF16)
            a1t_ref[:, rows] = a1.astype(BF16).T
            attn_ref[rows, :] = x_ref[rows, :].astype(F32) + rows_ref[5:6, :]

    @pl.loop(0, n // step)
    def _(b):
        rows = pl.ds(pl.multiple_of(b * step, step), step)
        a1 = a1_ref[rows, :]
        q = (dot_nn(a1, g_ref[0, 0]) + bqv_ref[0, 0:1, :]).astype(BF16)
        q_ref[0, rows, :] = q * jnp.asarray(HEAD_DIM ** -0.5, BF16)
        k = dot_nn(a1, g_ref[0, 1]).astype(BF16)
        k_ref[rows, :] = k
        kt_ref[0, :, rows] = k.T
        v = (dot_nn(a1, g_ref[0, 2]) + bqv_ref[0, 1:2, :]).astype(BF16)
        v_ref[0, rows, :] = v
        vt_ref[:, rows] = v.T

    for h in range(heads):
        k = k_ref[...]
        k = jnp.where(head_mask(k.shape, h), k, jnp.zeros_like(k))
        for b in range(n // step):
            first, last = b * step, (b + 1) * step
            q = q_ref[0, first:last, :]
            key = lax.broadcasted_iota(jnp.int32, (last, step), 0)
            query = lax.broadcasted_iota(jnp.int32, (step, step), 1) + first
            s = dot_nt(k[:last], q)
            near = jnp.where(
                (key[first:] <= query) & (key[first:] < length), s[first:], MASKED
            )
            if b:
                far = jnp.where(key[:first] < length, s[:first], MASKED)
                top = jnp.maximum(
                    jnp.max(far, 0, keepdims=True), jnp.max(near, 0, keepdims=True)
                )
                e_far = jnp.exp(far - top)
                e_near = jnp.exp(near - top)
                total = jnp.sum(e_far, 0, keepdims=True) + jnp.sum(e_near, 0, keepdims=True)
                scale = 1.0 / total
                p_ref[0, h, :first, first:last] = (e_far * scale).astype(BF16)
            else:
                top = jnp.max(near, 0, keepdims=True)
                e_near = jnp.exp(near - top)
                scale = 1.0 / jnp.sum(e_near, 0, keepdims=True)
            p_ref[0, h, first:last, first:last] = (e_near * scale).astype(BF16)
            ot_ref[h * HEAD_DIM : (h + 1) * HEAD_DIM, first:last] = dot_nn(
                vt_ref[h * HEAD_DIM : (h + 1) * HEAD_DIM, :last],
                p_ref[0, h, :last, first:last],
            ).astype(BF16)

    @pl.loop(0, n // step)
    def _(b):
        rows = pl.ds(pl.multiple_of(b * step, step), step)
        o = ot_ref[:, rows].T
        o_ref[0, rows, :] = o
        attn_ref[rows, :] += dot_nt(o, g_ref[0, 3])

    @pl.when(t == pl.num_programs(0) - 1)
    def _():
        @pl.loop(0, n // step)
        def _(b):
            rows = pl.ds(pl.multiple_of(b * step, step), step)
            h1 = attn_ref[rows, :]
            h1_ref[rows, :] = h1
            xhat, _ = norm_parts(h1)
            a2 = (xhat * rows_ref[1:2, :] + rows_ref[6:7, :]).astype(BF16)
            a2_ref[rows, :] = a2
            a2t_ref[:, rows] = a2.T


SQRT_2_PI = 0.7978845608028654


def feed_forward_both(
    len_ref, c_ref, a2_ref, a2t_ref, h1_ref, w1_ref, w2_ref, rows_ref,
    out_ref, d1_ref, d2_ref, dh1_ref, gb_ref, gbt_ref, sums_ref,
    gf_ref, gft_ref, feed_ref, da2_ref, h_ref, df_ref,
):
    t = pl.program_id(0)
    n = c_ref.shape[0]
    step = 256
    length = len_ref[0]

    @pl.when(t == 0)
    def _():
        sums_ref[...] = jnp.zeros_like(sums_ref)

        @pl.loop(0, n // step)
        def _(b):
            rows = pl.ds(pl.multiple_of(b * step, step), step)
            place = b * step + lax.broadcasted_iota(jnp.int32, (step, 1), 0)
            live = (place < length).astype(F32)
            g = (c_ref[rows, :].astype(F32) * live).astype(BF16)
            gf_ref[rows, :] = g
            gft_ref[:, rows] = g.T
            sums_ref[7:8, :] += jnp.sum(g.astype(F32), 0, keepdims=True)

    bias = rows_ref[pl.ds(8 + t, 1), :]

    @pl.loop(0, n // step)
    def _(b):
        rows = pl.ds(pl.multiple_of(b * step, step), step)
        f = dot_nn(a2_ref[rows, :], w1_ref[0]) + bias
        dh = dot_nn(gf_ref[rows, :], w2_ref[0])
        f2 = f * f
        th = jnp.tanh(f * (SQRT_2_PI + (SQRT_2_PI * 0.044715) * f2))
        half = 0.5 + 0.5 * th
        h = (f * half).astype(BF16)
        slope = half + f * (0.5 - 0.5 * th * th) * (
            SQRT_2_PI + (3 * SQRT_2_PI * 0.044715) * f2
        )
        df = (dh * slope).astype(BF16)
        h_ref[rows, :] = h
        df_ref[rows, :] = df
        sums_ref[pl.ds(8 + t, 1), :] += jnp.sum(df.astype(F32), 0, keepdims=True)
        feed = dot_nt(h, w2_ref[0])
        da2 = dot_nt(df, w1_ref[0])

        @pl.when(t == 0)
        def _():
            feed_ref[rows, :] = feed
            da2_ref[rows, :] = da2

        @pl.when(t > 0)
        def _():
            feed_ref[rows, :] += feed
            da2_ref[rows, :] += da2

    @pl.loop(0, D // step)
    def _(b):
        rows = pl.ds(pl.multiple_of(b * step, step), step)
        d1_ref[0, rows, :] = dot_nn(a2t_ref[rows, :], df_ref[...]).astype(BF16)
        d2_ref[0, rows, :] = dot_nn(gft_ref[rows, :], h_ref[...]).astype(BF16)

    @pl.when(t == pl.num_programs(0) - 1)
    def _():
        @pl.loop(0, n // step)
        def _(b):
            rows = pl.ds(pl.multiple_of(b * step, step), step)
            place = b * step + lax.broadcasted_iota(jnp.int32, (step, 1), 0)
            live = (place < length).astype(F32)
            h1 = h1_ref[rows, :]
            out_ref[rows, :] = (live * (h1 + (feed_ref[rows, :] + rows_ref[7:8, :]))).astype(BF16)
            xhat, r = norm_parts(h1)
            da2 = da2_ref[rows, :]
            sums_ref[1:2, :] += jnp.sum(da2 * xhat, 0, keepdims=True)
            sums_ref[6:7, :] += jnp.sum(da2, 0, keepdims=True)
            dg = da2 * rows_ref[1:2, :]
            dv = r * (
                dg
                - jnp.mean(dg, -1, keepdims=True)
                - xhat * jnp.mean(dg * xhat, -1, keepdims=True)
            )
            dh1 = live * c_ref[rows, :].astype(F32) + dv
            dh1_ref[rows, :] = dh1
            gb = dh1.astype(BF16)
            gb_ref[rows, :] = gb
            gbt_ref[:, rows] = gb.T
            sums_ref[5:6, :] += jnp.sum(gb.astype(F32), 0, keepdims=True)


def attention_backward(
    x_ref, g_ref, rows_ref, dh1_ref, gb_ref, gbt_ref, q_ref, v_ref, kt_ref, p_ref,
    o_ref, a1t_ref,
    d0_ref, xg_ref, sums_ref, bqv_ref,
    do_ref, delta_ref, dqt_ref, dq_ref, dk_ref, dv_ref, da1_ref,
):
    t = pl.program_id(0)
    n = x_ref.shape[0]
    width = g_ref.shape[-1]
    heads = width // HEAD_DIM
    step = 256
    pick = (
        lax.broadcasted_iota(jnp.int32, (16, width), 1) // HEAD_DIM
        == lax.broadcasted_iota(jnp.int32, (16, width), 0)
    ).astype(BF16)

    @pl.loop(0, n // step)
    def _(b):
        rows = pl.ds(pl.multiple_of(b * step, step), step)
        do = dot_nn(gb_ref[rows, :], g_ref[0, 3]).astype(BF16)
        do_ref[rows, :] = do
        prod = do.astype(F32) * o_ref[0, rows, :].astype(F32)
        high = prod.astype(BF16)
        low = (prod - high.astype(F32)).astype(BF16)
        delta_ref[:, rows] = dot_nt(pick, high) + dot_nt(pick, low)

    dqt_ref[...] = jnp.zeros_like(dqt_ref)
    for b in range(n // step):
        first, last = b * step, (b + 1) * step
        do = do_ref[first:, :]
        q = q_ref[0, first:, :]
        v = v_ref[0, first:last, :]
        dk, dv = None, None
        for h in range(heads):
            mine = head_mask((1, width), h)
            zero = jnp.zeros((), BF16)
            p = p_ref[0, h, first:last, first:]
            dp = dot_nt(jnp.where(mine, v, zero), do)
            ds = (p.astype(F32) * (dp - delta_ref[h : h + 1, first:])).astype(BF16)
            part = dot_nn(p, jnp.where(mine, do, zero))
            dv = part if dv is None else dv + part
            part = dot_nn(ds, jnp.where(mine, q, zero))
            dk = part if dk is None else dk + part
            head = slice(h * HEAD_DIM, (h + 1) * HEAD_DIM)
            dqt_ref[head, first:] += dot_nn(kt_ref[0, head, first:last], ds)
        dk_ref[first:last, :] = dk.astype(BF16)
        dv_ref[first:last, :] = dv.astype(BF16)

    @pl.when(t == 0)
    def _():
        da1_ref[...] = jnp.zeros_like(da1_ref)

    bqv_ref[...] = jnp.zeros_like(bqv_ref)

    @pl.loop(0, n // step)
    def _(b):
        rows = pl.ds(pl.multiple_of(b * step, step), step)
        dq = (dqt_ref[:, rows] * HEAD_DIM ** -0.5).astype(BF16).T
        dk = dk_ref[rows, :]
        dv = dv_ref[rows, :]
        dq_ref[rows, :] = dq
        bqv_ref[0, 0:1, :] += jnp.sum(dq.astype(F32), 0, keepdims=True)
        bqv_ref[0, 1:2, :] += jnp.sum(dv.astype(F32), 0, keepdims=True)
        da1_ref[rows, :] += (
            dot_nt(dq, g_ref[0, 0]) + dot_nt(dk, g_ref[0, 1]) + dot_nt(dv, g_ref[0, 2])
        )

    @pl.loop(0, D // step)
    def _(b):
        rows = pl.ds(pl.multiple_of(b * step, step), step)
        a1t = a1t_ref[rows, :]
        d0_ref[0, 0, rows, :] = dot_nn(a1t, dq_ref[...]).astype(BF16)
        d0_ref[0, 1, rows, :] = dot_nn(a1t, dk_ref[...]).astype(BF16)
        d0_ref[0, 2, rows, :] = dot_nn(a1t, dv_ref[...]).astype(BF16)
        d0_ref[0, 3, rows, :] = dot_nn(gbt_ref[rows, :], o_ref[0]).astype(BF16)

    @pl.when(t == pl.num_programs(0) - 1)
    def _():
        sums_ref[...] = jnp.zeros_like(sums_ref)

        @pl.loop(0, n // step)
        def _(b):
            rows = pl.ds(pl.multiple_of(b * step, step), step)
            xhat, r = norm_parts(x_ref[rows, :].astype(F32))
            da1 = da1_ref[rows, :]
            sums_ref[0:1, :] += jnp.sum(da1 * xhat, 0, keepdims=True)
            sums_ref[1:2, :] += jnp.sum(da1, 0, keepdims=True)
            dg = da1 * rows_ref[0:1, :]
            dv = r * (
                dg
                - jnp.mean(dg, -1, keepdims=True)
                - xhat * jnp.mean(dg * xhat, -1, keepdims=True)
            )
            xg_ref[rows, :] = (dh1_ref[rows, :] + dv).astype(BF16)


def whole(*shape):
    return pl.BlockSpec(shape, lambda t: (0,) * len(shape))


def group(*shape):
    return pl.BlockSpec((1,) + shape, lambda t: (t,) + (0,) * len(shape))


def shaped(dtype, *shape):
    return jax.ShapeDtypeStruct(shape, dtype)


SMEM_WHOLE = pl.BlockSpec(memory_space=pltpu.SMEM)


def run_attention_forward(length, x, g0, rows, bqv):
    n = x.shape[0]
    groups, _, _, width = g0.shape
    heads = width // HEAD_DIM
    return pl.pallas_call(
        attention_forward,
        grid=(groups,),
        in_specs=[SMEM_WHOLE, whole(n, D), group(4, D, width), whole(16, D), group(2, width)],
        out_specs=[
            group(n, width), group(n, width), group(width, n), group(heads, n, n),
            group(n, width), whole(D, n), whole(n, D), whole(n, D), whole(D, n),
        ],
        out_shape=[
            shaped(BF16, groups, n, width), shaped(BF16, groups, n, width),
            shaped(BF16, groups, width, n), shaped(BF16, groups, heads, n, n),
            shaped(BF16, groups, n, width), shaped(BF16, D, n), shaped(F32, n, D),
            shaped(BF16, n, D), shaped(BF16, D, n),
        ],
        scratch_shapes=[
            pltpu.VMEM((n, D), BF16), pltpu.VMEM((n, width), BF16),
            pltpu.VMEM((width, n), BF16), pltpu.VMEM((width, n), BF16),
            pltpu.VMEM((n, D), F32),
        ],
        compiler_params=pltpu.CompilerParams(vmem_limit_bytes=VMEM_LIMIT),
        name="attention_forward",
    )(length, x, g0, rows, bqv)


def run_feed_forward(length, cot, a2, a2t, h1, g1, g2, rows):
    n = cot.shape[0]
    groups, _, width = g1.shape
    return pl.pallas_call(
        feed_forward_both,
        grid=(groups,),
        in_specs=[
            SMEM_WHOLE, whole(n, D), whole(n, D), whole(D, n), whole(n, D),
            group(D, width), group(D, width), whole(16, D),
        ],
        out_specs=[
            whole(n, D), group(D, width), group(D, width), whole(n, D), whole(n, D),
            whole(D, n), whole(16, D),
        ],
        out_shape=[
            shaped(BF16, n, D), shaped(BF16, groups, D, width), shaped(BF16, groups, D, width),
            shaped(F32, n, D), shaped(BF16, n, D), shaped(BF16, D, n), shaped(F32, 16, D),
        ],
        scratch_shapes=[
            pltpu.VMEM((n, D), BF16), pltpu.VMEM((D, n), BF16), pltpu.VMEM((n, D), F32),
            pltpu.VMEM((n, D), F32), pltpu.VMEM((n, width), BF16), pltpu.VMEM((n, width), BF16),
        ],
        compiler_params=pltpu.CompilerParams(vmem_limit_bytes=VMEM_LIMIT),
        name="feed_forward_both",
    )(length, cot, a2, a2t, h1, g1, g2, rows)


def run_attention_backward(x, g0, rows, dh1, gb, gbt, q, v, kt, p, o, a1t):
    n = x.shape[0]
    groups, _, _, width = g0.shape
    heads = width // HEAD_DIM
    return pl.pallas_call(
        attention_backward,
        grid=(groups,),
        in_specs=[
            whole(n, D), group(4, D, width), whole(16, D), whole(n, D), whole(n, D),
            whole(D, n), group(n, width), group(n, width), group(width, n),
            group(heads, n, n), group(n, width), whole(D, n),
        ],
        out_specs=[group(4, D, width), whole(n, D), whole(8, D), group(8, width)],
        out_shape=[
            shaped(BF16, groups, 4, D, width), shaped(BF16, n, D), shaped(F32, 8, D),
            shaped(F32, groups, 8, width),
        ],
        scratch_shapes=[
            pltpu.VMEM((n, width), BF16), pltpu.VMEM((16, n), F32), pltpu.VMEM((width, n), F32),
            pltpu.VMEM((n, width), BF16), pltpu.VMEM((n, width), BF16),
            pltpu.VMEM((n, width), BF16), pltpu.VMEM((n, D), F32),
        ],
        compiler_params=pltpu.CompilerParams(vmem_limit_bytes=VMEM_LIMIT),
        name="attention_backward",
    )(x, g0, rows, dh1, gb, gbt, q, v, kt, p, o, a1t)


Z_DEV, Y_DEV, X_DEV, C_DEV = 4, 2, 2, 2


class Place:
    def __init__(self):
        dp, self.t = lax.axis_index("dp"), lax.axis_index("tensor")
        self.dp = dp
        self.z, self.y = dp // 2, dp % 2
        self.x, self.c = self.t // 2, self.t % 2
        self.other_y = 1 - self.y
        self.zs = [
            self.z,
            self.z + 1 - 2 * (self.z % 2),
            self.z + 2 - 4 * (self.z // 2),
            3 - self.z,
        ]
        self.ts = [
            self.t,
            self.t + 1 - 2 * (self.t % 2),
            self.t + 2 - 4 * (self.t // 2),
            3 - self.t,
        ]
        self.to_z = [dict(dp=z * 2 + self.y) for z in self.zs]
        self.to_y = dict(dp=self.z * 2 + self.other_y)
        self.to_x = dict(tensor=self.ts[2])
        self.same_t = self.to_z[1:] + [dict(dp=z * 2 + self.other_y) for z in self.zs]
        self.same_dp = [dict(tensor=t) for t in self.ts[1:]]
        self.to_core = dict(tensor=self.ts[1])

    def group(self, k):
        return lax.select(
            k == 0, self.ts[0],
            lax.select(k == 1, self.ts[1], lax.select(k == 2, self.ts[2], self.ts[3])),
        )

    def greet(self, others=None):
        barrier = pltpu.get_barrier_semaphore()
        others = others or self.to_z[1:] + [self.to_y, self.to_x, self.to_core]
        for device in others:
            pl.semaphore_signal(
                barrier, inc=1, device_id=device, device_id_type=pl.DeviceIdType.MESH
            )
        pl.semaphore_wait(barrier, len(others))


class Pieces:
    def __init__(self, whole, pieces):
        self.whole, self.pieces = whole, pieces

    def start(self):
        for piece in self.pieces:
            piece.start()

    def wait_recv(self):
        self.whole.wait_recv()

    def wait_send(self):
        self.whole.wait_send()


class Links:
    def __init__(self, send_sem, recv_sem):
        self.send_sem, self.recv_sem = send_sem, recv_sem
        self.copies = []

    def add(self, device, src, dst, parts=1, axis=0):
        number = len(self.copies)

        def make(src, dst):
            return pltpu.make_async_remote_copy(
                src_ref=src,
                dst_ref=dst,
                send_sem=self.send_sem.at[number],
                recv_sem=self.recv_sem.at[number],
                device_id=device,
                device_id_type=pl.DeviceIdType.MESH,
            )

        size = src.shape[axis] // parts
        cuts = [(slice(None),) * axis + (pl.ds(i * size, size),) for i in range(parts)]
        copy = Pieces(make(src, dst), [make(src.at[cut], dst.at[cut]) for cut in cuts])
        self.copies.append(copy)
        return copy

    def sent(self, *apart):
        for copy in self.copies:
            if all(copy is not other for other in apart):
                copy.wait_send()


def flat(copies):
    for item in copies:
        if isinstance(item, list):
            yield from flat(item)
        else:
            yield item


def start(*copies):
    for copy in flat(copies):
        copy.start()


def recv(*copies):
    for copy in flat(copies):
        copy.wait_recv()


class Gather:
    def __init__(self, links, place, own, full, order, single=True, last=True):
        every = slice(None)
        y, other = place.y, place.other_y

        def same(device, k, yy, to):
            return links.add(device, full(k, every, yy), full(to, every, yy), Z_DEV)

        def along_z(k, yy, block):
            here, passed = full(k, place.z, yy), full(k, place.zs[2], yy)
            return [
                links.add(place.to_z[1], block, here),
                links.add(place.to_z[2], block, here),
                links.add(place.to_z[1], passed, passed),
            ]

        if order != WHOLE:
            self.z = along_z(0, y, own)
        if order == X_Z_Y:
            self.first = [links.add(place.to_x, own, full(2, place.z, y), 2)]
            self.far = along_z(2, y, full(2, place.z, y))
            blocks = [(0, y), (2, y), (0, other), (2, other)]
        else:
            blocks = [(0, y), (0, other), (2, y), (2, other)]
        if order == Y_Z_X:
            self.first = [links.add(place.to_y, own, full(0, place.z, y), 2)]
            self.far = along_z(0, other, full(0, place.z, other))
        if order == Z_Y_X and single:
            self.first = [same(place.to_y, 0, y, 0)]
        if order == Z_Y_X and not single:
            self.first = [links.add(place.to_y, own, full(0, place.z, y))]
            for k in range(1, 4):
                block = full(0, place.zs[k], y)
                self.first.append(links.add(place.to_y, block, block))
            return
        self.second = [
            same(place.to_y, k, yy, k) if order == X_Z_Y else same(place.to_x, k, yy, 2)
            for k, yy in blocks[: 2 if last else 1]
        ]
        if not last:
            blocks = [block for block in blocks if block[0] == 0]
        self.core = [same(place.to_core, k, yy, k + 1) for k, yy in blocks]


Z_Y_X, Y_Z_X, X_Z_Y, WHOLE = range(4)


def fused_forward(
    tie_ref, len_ref, tokens_ref, gains_ref, bias_ref, in_ref, out_ref, expand_ref,
    project_ref,
    gq_ref, gw_ref, flat1_ref, flat2_ref, rows_ref,
    q_ref, v_ref, kt_ref, p_ref, scale_ref, o_ref, a1t_out, h1_out, a2_out, a2t_out,
    own0_ref, ownw_ref, own1_ref, own2_ref, square_ref, vec_ref,
    all0_ref, allw_ref, w1_ref, w2_ref, vecs_ref, bqv_ref, x_ref, a1_ref, k_ref, qa_ref, vt_ref, ot_ref, a1t_ref, h1_ref, a2_ref, a2t_ref,
    send_sem, recv_sem, local_sem, flush_sem, row_sem,
):
    t, h = pl.program_id(0), pl.program_id(1)
    n, _ = x_ref.shape
    width = allw_ref.shape[-1]
    heads = width // HEAD_DIM
    step = 256
    place = Place()
    length = len_ref[place.t]
    links = Links(send_sem, recv_sem)
    z, y, x, c = place.z, place.y, place.x, place.c
    mine_there = vecs_ref.at[z, y, x, c]
    column = vecs_ref.at[:, :, x, c]
    vec_one = [links.add(device, vec_ref, mine_there) for device in place.same_t]
    vec_two = [links.add(device, column, column) for device in place.same_dp]
    half = own0_ref.shape[0] // 2
    halves = []
    for i in range(2):
        rows = pl.ds(i * half, half)
        halves.append(Gather(
            links, place, own0_ref.at[rows],
            lambda k, z, y, rows=rows: all0_ref.at[k, z, y, rows], Z_Y_X, single=False,
        ))
    seg0 = Gather(links, place, own0_ref, lambda k, z, y: all0_ref.at[k, z, y], WHOLE)
    segw = Gather(links, place, ownw_ref, lambda k, z, y: allw_ref.at[k, z, y], Z_Y_X)
    seg1 = Gather(
        links, place, own1_ref, lambda k, z, y: w1_ref.at[k, z, y], Y_Z_X, last=False
    )
    seg2 = Gather(
        links, place, own2_ref, lambda k, z, y: w2_ref.at[k, z, y], X_Z_Y, last=False
    )
    flush = [
        [
            pltpu.make_async_copy(ref.at[k], flat.at[k], flush_sem.at[i, k])
            for k in range(3)
        ]
        for i, (ref, flat) in enumerate([(w1_ref, flat1_ref), (w2_ref, flat2_ref)])
    ]
    put_a1t = pltpu.make_async_copy(a1t_ref, a1t_out, local_sem.at[0])
    put_a2t = pltpu.make_async_copy(a2t_ref, a2t_out, local_sem.at[1])
    puts = []
    for i in range(n // step):
        rows = pl.ds(i * step, step)
        puts.append([
            pltpu.make_async_copy(h1_ref.at[rows], h1_out.at[rows], row_sem.at[0, i]),
            pltpu.make_async_copy(a2_ref.at[rows], a2_out.at[rows], row_sem.at[1, i]),
        ])
    fetch = pltpu.make_async_copy(tokens_ref.at[place.t], x_ref, local_sem.at[2])

    def relay_z(copies):
        recv(copies[1])
        start(copies[2])

    def pass_own(seg):
        recv(seg.z[0], seg.z[2])
        if seg is segw:
            start(seg.first)
        start(seg.second[0], seg.core[0])

    def pass_second(seg):
        recv(seg.second)
        if seg is seg2:
            start(seg.core[1])

    def pass_first(seg):
        recv(seg.first)
        if seg is segw:
            start(seg.second[1], seg.core[1])
        else:
            start(seg.far[1], seg.far[0])

    def pass_far(seg):
        recv(seg.far[0], seg.far[2])
        start(seg.core[1:] if seg is seg1 else [])

    def pass_core(seg, i):
        recv(seg.second[i])
        start(seg.core[2 + i])

    plan = [
        (0, 0, lambda: (pass_own(segw), pass_first(seg1), relay_z(seg2.z), pass_first(seg2))),
        (0, 3, lambda: (pass_first(segw), relay_z(seg1.z), pass_core(seg0, 0))),
        (1, 0, lambda: recv(seg0.core[:2])),
        (1, 1, lambda: relay_z(seg1.far)),
        (1, 3, lambda: pass_core(seg0, 1)),
        (1, 4, lambda: (recv(segw.core[:2]), pass_core(segw, 0), pass_own(seg2))),
        (2, 1, lambda: relay_z(seg2.far)),
        (2, 2, lambda: pass_core(segw, 1)),
        (2, 3, lambda: pass_own(seg1)),
        (3, 0, lambda: (recv(seg0.core[2:]), pass_far(seg1), flush[0][0].start())),
        (3, 2, lambda: (pass_second(seg2), flush[1][0].start())),
        (3, 3, lambda: (pass_far(seg2), flush[1][2].start())),
        (3, 4, lambda: recv(segw.core[2:])),
    ]

    def serve(points):
        for step, where, act in plan:
            if where in points:
                now = (t == step) & (h == max(where - 2, 0))
                pl.when(now)(lambda act=act: (act(), None)[1])

    @pl.when((t == 0) & (h == 0))
    def _():
        s0, s1, s2, s3 = tie_ref[0], tie_ref[1], tie_ref[2], tie_ref[3]
        fetch.start()
        square_ref[...] = jnp.zeros_like(square_ref)
        gain = gains_ref.shape[-1]
        square_ref[0:1, :gain] = gains_ref[s0].astype(F32)[0:1]
        square_ref[1:2, :gain] = gains_ref[s2].astype(F32)[1:2]
        kinds = [s0, s0, s0, s1, s2, s3, s2, s2, s2, s2]
        for i, source in enumerate(kinds):
            wide = bias_ref[i].astype(F32)
            here = lax.broadcasted_iota(jnp.int32, wide.shape, 0) == source
            square_ref[2 + i : 3 + i, :gain] = jnp.sum(
                jnp.where(here, wide, 0.0), 0, keepdims=True
            )
        vec_ref[...] = square_ref[...].T[:gain]
        for j in range(3):
            own0_ref[:, j * width : (j + 1) * width] = in_ref[s0, j]
        place.greet(place.same_t + place.same_dp)
        start(vec_one)
        for part in halves:
            start(part.z[1], part.z[0], part.first[0])
        vecs_ref[z, y, x, c] = vec_ref[...]
        ones = lax.broadcasted_iota(jnp.int32, (vt_ref.shape[1] - HEAD_DIM, n), 0) == 0
        for h in range(heads):
            vt_ref[h, HEAD_DIM:, :] = ones.astype(BF16)
        all0_ref[0, z, y] = own0_ref[...]
        ownw_ref[...] = out_ref[s1].T
        allw_ref[0, z, y] = ownw_ref[...]
        own1_ref[...] = expand_ref[s2]
        own2_ref[...] = project_ref[s3]
        w1_ref[0, z, y] = own1_ref[...]
        w2_ref[0, z, y] = own2_ref[...]
        recv(vec_one)
        start(vec_two)
        for part in halves:
            relay_z(part.z)
            start(part.first[2])
        for part in halves:
            recv(part.z[0])
            start(part.first[1])
        start(segw.z[1], segw.z[0], seg2.z[1])
        recv(vec_two)
        start(seg2.first)
        vecs = vecs_ref[...].reshape(D, vecs_ref.shape[-1]).T[:16]
        rows_ref[...] = vecs
        for part in halves:
            recv(part.z[2])
            start(part.first[3])
        start(seg1.first, seg0.second[0], seg0.core[0])
        for k in range(4):
            part = slice(k * width, (k + 1) * width)
            bqv_ref[k, 0:1, :width] = vecs[3:4, part]
            bqv_ref[k, 0:1, width : 2 * width] = jnp.zeros((1, width), F32)
            bqv_ref[k, 0:1, 2 * width :] = vecs[4:5, part]
        fetch.wait()

        @pl.loop(0, n // step)
        def _(b):
            rows = pl.ds(pl.multiple_of(b * step, step), step)
            wide = x_ref[rows, :].astype(F32)
            xhat, _ = norm_parts(wide)
            a1 = (xhat * rows_ref[0:1, :] + rows_ref[2:3, :]).astype(BF16)
            a1_ref[rows, :] = a1
            a1t_ref[:, rows] = a1.T
            h1_ref[rows, :] = wide + rows_ref[5:6, :]

        put_a1t.start()
        relay_z(segw.z)
        start(seg2.z[0], seg1.z[1], seg1.z[0])
        recv(halves[0].first, halves[1].first)
        start(seg0.second[1], seg0.core[1])

    serve([0])

    @pl.when(h == 0)
    def _():
        gq = all0_ref[t].reshape(D, 3 * width)
        gq_ref[0] = gq
        mine = place.group(t)
        qkv = dot_nn(a1_ref[...], gq) + bqv_ref[mine, 0:1, :]
        q = qkv[:, :width].astype(BF16) * jnp.asarray(HEAD_DIM ** -0.5, BF16)
        k = qkv[:, width : 2 * width].astype(BF16)
        v = qkv[:, 2 * width :].astype(BF16)
        q_ref[0] = q
        kt_ref[0] = k.T
        v_ref[0] = v
        vt = v.T
        for h in range(heads):
            vt_ref[h, :HEAD_DIM, :] = vt[h * HEAD_DIM : (h + 1) * HEAD_DIM]
        spare = k_ref.shape[1] - width
        dead = lax.broadcasted_iota(jnp.int32, (n, spare), 0) >= length
        first_column = lax.broadcasted_iota(jnp.int32, (n, spare), 1) == 0
        k_ref[:, :width] = k
        k_ref[:, width:] = jnp.where(first_column & dead, MASKED, 0.0).astype(BF16)
        qa_ref[:, :width] = q
        qa_ref[:, width:] = jnp.where(first_column, 1.0, 0.0).astype(BF16)
        scale_ref[0, heads:, :] = jnp.zeros((scale_ref.shape[1] - heads, n), F32)

    serve([1])

    lane = lax.broadcasted_iota(jnp.int32, (1, qa_ref.shape[1]), 1)
    keep = ((lane >= h * HEAD_DIM) & (lane < (h + 1) * HEAD_DIM)) | (lane >= width)
    key = lax.broadcasted_iota(jnp.int32, (step, step), 0)
    query = lax.broadcasted_iota(jnp.int32, (step, step), 1)
    head = pl.ds(pl.multiple_of(h * HEAD_DIM, HEAD_DIM), HEAD_DIM)

    def scores(b):
        first, last = b * step, (b + 1) * step
        q = jnp.where(keep, qa_ref[first:last, :], jnp.zeros((), BF16))
        return dot_nt(k_ref[:last, :], q)

    def attend(b, s):
        first, last = b * step, (b + 1) * step
        near = jnp.where(key <= query, s[first:], MASKED)
        top = jnp.max(near, 0, keepdims=True)
        if b:
            far = s[:first]
            top = jnp.maximum(top, jnp.max(far, 0, keepdims=True))
        e_near = jnp.exp((near - top).astype(BF16))
        p_ref[0, 0, b, first:last, :] = e_near
        o = dot_nn(vt_ref[h, :, first:last], e_near)
        if b:
            e_far = jnp.exp((far - top).astype(BF16))
            p_ref[0, 0, b, :first, :] = e_far
            o += dot_nn(vt_ref[h, :, :first], e_far)
        scale = 1.0 / o[HEAD_DIM : HEAD_DIM + 1]
        scale_ref[0, pl.ds(h, 1), first:last] = scale
        ot_ref[head, first:last] = (o[:HEAD_DIM] * scale).astype(BF16)

    s = scores(0)
    for b in range(n // step):
        ahead = scores(b + 1) if b + 1 < n // step else None
        attend(b, s)
        s = ahead

    serve([2, 3, 4])

    @pl.when(h == heads - 1)
    def _():
        gw_ref[0] = allw_ref[t].reshape(gw_ref.shape[1:])
        o = ot_ref[...].T
        o_ref[0] = o
        h1_ref[...] += dot_nt(o, gw_ref[0])

    @pl.when((t == 3) & (h == heads - 1))
    def _():
        for i, rows in enumerate(blocks(n, step)):
            xhat, _ = norm_parts(h1_ref[rows, :])
            a2 = (xhat * rows_ref[1:2, :] + rows_ref[6:7, :]).astype(BF16)
            a2_ref[rows, :] = a2
            a2t_ref[:, rows] = a2.T
            for put in puts[i]:
                put.start()
        put_a2t.start()
        recv(seg2.core)
        flush[1][1].start()
        recv(seg1.core)
        flush[0][1].start()
        pass_second(seg1)
        flush[0][2].start()
        links.sent()
        for copies in flush + puts + [[put_a1t, put_a2t]]:
            for copy in copies:
                copy.wait()


N_GATHER = 10 + 14 + 6 + 10 + 10 + 10
VMEM_WHOLE = pl.BlockSpec(memory_space=pltpu.VMEM)
ANY_WHOLE = pl.BlockSpec(memory_space=pl.ANY)


def run_fused_forward(tie, lengths, tokens, gains, biases, w_in, w_out, w_expand, w_project):
    groups, n, _ = tokens.shape
    depth, width = w_in.shape[-2:]
    heads = width // HEAD_DIM
    hidden = w_expand.shape[-1]
    w_project = w_project.transpose(0, 2, 1)
    biases = biases.transpose(1, 0, 2)
    own = gains.shape[-1]

    def group(*shape):
        return pl.BlockSpec((1,) + shape, lambda t, h: (t,) + (0,) * len(shape))

    per_head = pl.BlockSpec((1, 1, n // 256, n, 256), lambda t, h: (t, h, 0, 0, 0))
    return pl.pallas_call(
        fused_forward,
        grid=(groups, heads),
        in_specs=[SMEM_WHOLE, SMEM_WHOLE, ANY_WHOLE] + [VMEM_WHOLE] * 6,
        out_specs=[
            group(D, 3 * width), group(D, width), ANY_WHOLE, ANY_WHOLE, VMEM_WHOLE,
            group(n, width), group(n, width), group(width, n), per_head,
            group(8, n), group(n, width), ANY_WHOLE, ANY_WHOLE, ANY_WHOLE, ANY_WHOLE,
        ],
        out_shape=[
            shaped(BF16, groups, D, 3 * width), shaped(BF16, groups, D, width),
            shaped(BF16, groups, Z_DEV, Y_DEV, depth, hidden),
            shaped(BF16, groups, Z_DEV, Y_DEV, depth, hidden),
            shaped(F32, 16, D),
            shaped(BF16, groups, n, width), shaped(BF16, groups, n, width),
            shaped(BF16, groups, width, n), shaped(BF16, groups, heads, n // 256, n, 256),
            shaped(F32, groups, 8, n), shaped(BF16, groups, n, width), shaped(BF16, D, n), shaped(F32, n, D),
            shaped(BF16, n, D), shaped(BF16, D, n),
        ],
        scratch_shapes=[
            pltpu.VMEM((depth, 3 * width), BF16), pltpu.VMEM((depth, width), BF16),
            pltpu.VMEM((depth, hidden), BF16), pltpu.VMEM((depth, hidden), BF16),
            pltpu.VMEM((128, 128), F32), pltpu.VMEM((own, 128), F32),
            pltpu.VMEM((groups, Z_DEV, Y_DEV, depth, 3 * width), BF16),
            pltpu.VMEM((groups, Z_DEV, Y_DEV, depth, width), BF16),
            pltpu.VMEM((groups, Z_DEV, Y_DEV, depth, hidden), BF16),
            pltpu.VMEM((groups, Z_DEV, Y_DEV, depth, hidden), BF16),
            pltpu.VMEM((Z_DEV, Y_DEV, X_DEV, C_DEV, own, 128), F32),
            pltpu.VMEM((groups, 8, 3 * width), F32),
            pltpu.VMEM((n, D), BF16), pltpu.VMEM((n, D), BF16), pltpu.VMEM((n, 256), BF16),
            pltpu.VMEM((n, 256), BF16), pltpu.VMEM((heads, HEAD_DIM + 16, n), BF16),
            pltpu.VMEM((width, n), BF16),
            pltpu.VMEM((D, n), BF16), pltpu.VMEM((n, D), F32), pltpu.VMEM((n, D), BF16),
            pltpu.VMEM((D, n), BF16),
            pltpu.SemaphoreType.DMA((N_GATHER,)), pltpu.SemaphoreType.DMA((N_GATHER,)),
            pltpu.SemaphoreType.DMA((3,)), pltpu.SemaphoreType.DMA((2, 4)),
            pltpu.SemaphoreType.DMA((2, n // 256)),
        ],
        compiler_params=pltpu.CompilerParams(
            vmem_limit_bytes=VMEM_LIMIT, collective_id=0, has_side_effects=True
        ),
        name="fused_forward",
    )(tie, lengths, tokens, gains, biases, w_in, w_out, w_expand, w_project)


class Result:
    def __init__(self, links, place, own_ref, passing_ref, out_ref, step, sem, count):
        self.x, self.core, self.far, self.keep, self.keep_far = [], [], [], [], []
        for i in range(count):
            rows = pl.ds(i * step, step)
            mine, theirs = out_ref.at[place.t, rows], out_ref.at[place.ts[2], rows]
            own, passing = own_ref.at[rows], passing_ref.at[rows]
            self.x.append(links.add(place.to_x, own, passing))
            self.core.append(links.add(place.to_core, own, mine))
            self.far.append(links.add(place.to_core, passing, theirs))
            self.keep.append(pltpu.make_async_copy(own, mine, sem.at[0, i]))
            self.keep_far.append(pltpu.make_async_copy(passing, theirs, sem.at[1, i]))

    def send(self, i):
        start(self.x[i], self.core[i], self.keep[i])

    def pass_on(self, i):
        recv(self.x[i])
        start(self.far[i], self.keep_far[i])

    def finish(self):
        recv(self.core, self.far)
        for copy in self.keep + self.keep_far:
            copy.wait()


def low(value):
    return jnp.asarray(value, BF16)


def pair_order(i):
    return i + 1 - 2 * (i % 2)


def fused_feed_forward(
    len_ref, cot_ref, a2_ref, a2t_in, h1_in, far1_ref, far2_ref, rows_ref,
    result_out, rest_out, fold_ref, work_out, dh1_out, gb_out, gbt_out, sums_ref,
    gf_ref, gft_ref, feed_ref, da2_ref, h_ref, df_ref, weights_ref, missing_ref, third_ref,
    stage_ref, land_ref, near_ref, cross_ref, a2t_ref, h1_ref, out_ref, work_ref,
    passing_ref, send_sem, recv_sem, local_sem, row_sem, result_sem,
):
    t = pl.program_id(0)
    n = gf_ref.shape[0]
    step = 256
    depth = stage_ref.shape[-2]
    place = Place()
    length = len_ref[place.t]
    links = Links(send_sem, recv_sem)
    y, other = place.y, place.other_y
    last = [
        links.add(place.to_x, far1_ref.at[0, :, other], missing_ref.at[0, 0], Z_DEV),
        links.add(place.to_y, far2_ref.at[2, :, y], missing_ref.at[1, 0], Z_DEV),
    ]
    last_core = [
        links.add(place.to_core, missing_ref.at[i, 0], missing_ref.at[i, 1], Z_DEV)
        for i in range(2)
    ]
    third = [
        links.add(place.to_core, far_ref.at[2, :, y], third_ref.at[i], Z_DEV)
        for i, far_ref in enumerate([far1_ref, far2_ref])
    ]
    core = [
        [
            links.add(place.to_core, stage_ref.at[i], land_ref.at[s, i], Z_DEV) for i in range(2)
        ]
        for s in range(2)
    ]
    cross = [
        links.add(place.to_y, near_ref.at[i, :, other], cross_ref.at[i], Z_DEV)
        for i in range(2)
    ]
    out = Result(links, place, out_ref, passing_ref, result_out, step, result_sem, 1)
    fetch = pltpu.make_async_copy(cot_ref.at[place.t], gf_ref, local_sem.at[0])
    gb_ref, gbt_ref, dh1_ref = gf_ref, gft_ref, da2_ref
    late = [
        pltpu.make_async_copy(a2t_in, a2t_ref, local_sem.at[5]),
        pltpu.make_async_copy(h1_in, h1_ref, local_sem.at[6]),
    ]
    puts = []
    for i in range(n // step):
        rows = pl.ds(i * step, step)
        puts.append([
            pltpu.make_async_copy(ref.at[rows], out.at[rows], row_sem.at[j, i])
            for j, (ref, out) in enumerate(
                [(dh1_ref, dh1_out), (gb_ref, gb_out)]
            )
        ])
    put_gbt = pltpu.make_async_copy(gbt_ref, gbt_out, local_sem.at[7])
    put_work = pltpu.make_async_copy(work_ref, work_out, local_sem.at[8])
    put_rest = pltpu.make_async_copy(
        out_ref.at[pl.ds(step, n - step)], rest_out, local_sem.at[9]
    )
    k = pair_order(t)
    mine = place.group(k)

    def load(step, whole, slot):
        for i, far_ref in enumerate([far1_ref, far2_ref]):
            group = far_ref.at[pair_order(step)]
            to = weights_ref.at[slot, i]
            if not whole:
                group, to = group.at[:, y], to.at[:, y]
            yield pltpu.make_async_copy(group, to, local_sem.at[1 + 2 * slot + i])

    def live_rows(b):
        at = b * step + lax.broadcasted_iota(jnp.int32, (step, 1), 0)
        return (at < length).astype(F32)

    @pl.when(t == 0)
    def _():
        fetch.start()
        for copy in load(0, True, 0):
            copy.start()
        for copy in late:
            copy.start()
        place.greet()
        start(last, third)
        sums_ref[...] = jnp.zeros_like(sums_ref)
        feed_ref[...] = jnp.zeros_like(feed_ref)
        da2_ref[...] = jnp.zeros_like(da2_ref)
        fetch.wait()

        @pl.loop(0, n // step)
        def _(b):
            rows = pl.ds(pl.multiple_of(b * step, step), step)
            g = (gf_ref[rows, :].astype(F32) * live_rows(b)).astype(BF16)
            gf_ref[rows, :] = g
            gft_ref[:, rows] = g.T
            sums_ref[7:8, :] += jnp.sum(g.astype(F32), 0, keepdims=True)

    for i in range(4):
        @pl.when(t == i)
        def _():
            if i == 2:
                recv(last_core, third)
            else:
                for copy in load(i, i < 2, i % 2):
                    copy.wait()
            if i in (0, 2):
                for copy in load(i + 1, i + 1 < 2, (i + 1) % 2):
                    copy.start()
            for j in range(2):
                if i == 2:
                    weights_ref[0, j, :, y] = third_ref[j]
                if i >= 2:
                    weights_ref[i % 2, j, :, other] = missing_ref[j, 3 - i]

    bias = rows_ref[pl.ds(8 + mine, 1), :]
    w1 = weights_ref[t % 2, 0].reshape(D, -1)
    w2 = weights_ref[t % 2, 1].reshape(D, -1)

    def bend(f):
        f = f.astype(BF16)
        f2 = f * f
        th = jnp.tanh(f * (low(SQRT_2_PI) + low(SQRT_2_PI * 0.044715) * f2))
        half = low(0.5) + low(0.5) * th
        slope = half + f * (low(0.5) - low(0.5) * th * th) * (
            low(SQRT_2_PI) + low(3 * SQRT_2_PI * 0.044715) * f2
        )
        return f * half, slope

    column = jnp.zeros((1, w1.shape[1]), F32)
    for rows in blocks(n, step):
        f = dot_nn(a2_ref[rows, :], w1) + bias
        dh = dot_nn(gf_ref[rows, :], w2)
        h, slope = bend(f)
        df = (dh * slope.astype(F32)).astype(BF16)
        h_ref[rows, :] = h
        df_ref[rows, :] = df
        column += jnp.sum(df.astype(F32), 0, keepdims=True)
        feed_ref[rows, :] += dot_nt(h, w2)
        da2_ref[rows, :] += dot_nt(df, w1)
    sums_ref[pl.ds(8 + mine, 1), :] = column

    @pl.when(t == 3)
    def _():
        late[1].wait()
        for i, rows in enumerate(blocks(n, step)):
            total = h1_ref[rows, :] + (feed_ref[rows, :] + rows_ref[7:8, :])
            out_ref[rows, :] = (live_rows(i) * total).astype(BF16)
            if i == 0:
                out.send(0)
        put_rest.start()

    @pl.when(t == 1)
    def _():
        recv(last)
        start(last_core)

    @pl.when(t == 0)
    def _():
        late[0].wait()

    def weight_grad(left_ref, right_ref):
        value = dot_nn(left_ref[...], right_ref[...])
        return value.reshape(Z_DEV, Y_DEV, depth, value.shape[-1]).astype(BF16)

    grad1 = weight_grad(a2t_ref, df_ref)
    grad2 = weight_grad(gft_ref, h_ref)

    def put(ref):
        ref[0] = grad1
        ref[1] = grad2

    def reduced(ref):
        return lambda i, s, z: (
            ref[i, z].astype(F32) + land_ref[s, i, z].astype(F32)
        ).astype(BF16)

    @pl.when(t == 0)
    def _():
        put(stage_ref)
        start(core[0])

    @pl.when(t == 1)
    def _():
        put(near_ref)
        recv(core[0])

        @pl.loop(0, Z_DEV)
        def _(z):
            for i in range(2):
                near_ref[i, z] = reduced(near_ref)(i, 0, z)

        start(cross)

    @pl.when(t == 2)
    def _():
        for copy in core[0]:
            copy.wait_send()
        put(stage_ref)
        start(core[1])

    @pl.when(t == 3)
    def _():
        put(work_ref)
        for i, rows in enumerate(blocks(n, step)):
            xhat, r = norm_parts(h1_ref[rows, :])
            da2 = da2_ref[rows, :]
            sums_ref[1:2, :] += jnp.sum(da2 * xhat, 0, keepdims=True)
            sums_ref[6:7, :] += jnp.sum(da2, 0, keepdims=True)
            dg = da2 * rows_ref[1:2, :]
            dv = r * (
                dg
                - jnp.mean(dg, -1, keepdims=True)
                - xhat * jnp.mean(dg * xhat, -1, keepdims=True)
            )
            dh1 = gf_ref[rows, :].astype(F32) + dv
            dh1_ref[rows, :] = dh1
            gb = dh1.astype(BF16)
            gb_ref[rows, :] = gb
            gbt_ref[:, rows] = gb.T
            sums_ref[5:6, :] += jnp.sum(gb.astype(F32), 0, keepdims=True)
            for copy in puts[i]:
                copy.start()
        put_gbt.start()
        recv(core[1])

        @pl.loop(0, Z_DEV)
        def _(z):
            for i in range(2):
                work_ref[i, z] = reduced(work_ref)(i, 1, z)

        put_work.start()
        recv(cross)

        @pl.loop(0, Z_DEV)
        def _(z):
            for i in range(2):
                fold_ref[i, z] = (
                    near_ref[i, z, y].astype(F32) + cross_ref[i, z].astype(F32)
                ).astype(BF16)

        out.pass_on(0)
        out.finish()
        links.sent(*core[0])
        for copies in puts + [[put_gbt, put_work, put_rest]]:
            for copy in copies:
                copy.wait()


def run_fused_feed_forward(lengths, cot, a2, a2t, h1, g1, g2, rows):
    n = cot.shape[1]
    groups, _, _, depth, hidden = g1.shape
    both = (2, Z_DEV, Y_DEV, depth, hidden)
    fold = (2, Z_DEV, depth, hidden)
    return pl.pallas_call(
        fused_feed_forward,
        grid=(groups,),
        in_specs=[SMEM_WHOLE, ANY_WHOLE, VMEM_WHOLE] + [ANY_WHOLE] * 4 + [VMEM_WHOLE],
        out_specs=[ANY_WHOLE] * 2 + [VMEM_WHOLE] + [ANY_WHOLE] * 4 + [VMEM_WHOLE],
        out_shape=[
            shaped(BF16, groups, n // 4, D), shaped(BF16, n - n // 4, D), shaped(BF16, *fold),
            shaped(BF16, *both), shaped(F32, n, D),
            shaped(BF16, n, D), shaped(BF16, D, n), shaped(F32, 16, D),
        ],
        scratch_shapes=[
            pltpu.VMEM((n, D), BF16), pltpu.VMEM((D, n), BF16), pltpu.VMEM((n, D), F32),
            pltpu.VMEM((n, D), F32), pltpu.VMEM((n, hidden), BF16), pltpu.VMEM((n, hidden), BF16),
            pltpu.VMEM((2,) + both, BF16),
            pltpu.VMEM((2,) + fold, BF16), pltpu.VMEM(fold, BF16), pltpu.VMEM(both, BF16),
            pltpu.VMEM((2,) + both, BF16),
            pltpu.VMEM(both, BF16), pltpu.VMEM(fold, BF16),
            pltpu.VMEM((D, n), BF16), pltpu.VMEM((n, D), F32), pltpu.VMEM((n, D), BF16),
            pltpu.VMEM(both, BF16), pltpu.VMEM((n // 4, D), BF16),
            pltpu.SemaphoreType.DMA((15,)), pltpu.SemaphoreType.DMA((15,)),
            pltpu.SemaphoreType.DMA((10,)), pltpu.SemaphoreType.DMA((2, n // 256)),
            pltpu.SemaphoreType.DMA((2, 1)),
        ],
        compiler_params=pltpu.CompilerParams(
            vmem_limit_bytes=VMEM_LIMIT, collective_id=1, has_side_effects=True
        ),
        name="fused_feed_forward",
    )(lengths, cot, a2, a2t, h1, g1, g2, rows)
class Reduce:
    def __init__(
        self, links, place, work, acc, cross_ref, far_ref, mid_ref, last_ref, side_ref,
        slots=(0, 1),
    ):
        self.place, self.work, self.acc = place, work, acc
        self.cross_ref, self.far_ref, self.mid_ref = cross_ref, far_ref, mid_ref
        self.last_ref, self.side_ref = last_ref, side_ref
        zs = place.zs
        self.y = {
            s: [
                links.add(
                    place.to_y, work(s, zs[j], place.other_y), cross_ref.at[s, zs[j]], 2
                )
                for j in (1, 3, 2, 0)
            ]
            for s in slots
        }
        self.z = [
            [
                links.add(place.to_z[1], acc(s, zs[1]), far_ref.at[s, 0], 2),
                links.add(place.to_z[1], acc(s, zs[3]), far_ref.at[s, 1], 2),
                links.add(place.to_z[2], mid_ref.at[s, 1], far_ref.at[s, 2], 2),
            ]
            for s in range(2)
        ]
        self.x = links.add(place.to_x, last_ref, side_ref, 2)

    def fold_y(self, s, half):
        for i, j in [(0, 1), (1, 3), (2, 2), (3, 0)][2 * half : 2 * half + 2]:
            z = self.place.zs[j]
            recv(self.y[s][i])
            value = self.work(s, z, self.place.y)[...].astype(F32)
            self.acc(s, z)[...] = (value + self.cross_ref[s, z].astype(F32)).astype(BF16)
            if i < 2:
                start(self.z[s][i])

    def fold_z(self, s):
        recv(self.z[s][:2])
        for i in (1, 0):
            value = self.acc(s, self.place.zs[2 * i])[...].astype(F32)
            self.mid_ref[s, i] = (value + self.far_ref[s, i].astype(F32)).astype(BF16)
            if i:
                start(self.z[s][2])

    def own(self, s):
        recv(self.z[s][2])
        return self.mid_ref[s, 0].astype(F32) + self.far_ref[s, 2].astype(F32)

    def send_x(self):
        self.last_ref[...] = self.own(1).astype(BF16)
        start(self.x)

    def total(self):
        value = self.own(0)
        recv(self.x)
        return value + self.side_ref[...].astype(F32)


def fused_backward(
    tokens_ref, gq_in, gw_in, rows_ref, dh1_ref, gb_ref, gbt_in, q_in, v_in, kt_in,
    p_ref, scale_in, o_in, a1t_in, layer_in, fold_in, work_in, early_ref,
    out_ref, layerout_ref, part0_ref, partw_ref, part1_ref, part2_ref, total_ref,
    gq_ref, gw_ref, q_ref, v_ref, kt_ref, scale_ref, o_ref,
    a1t_ref, gbt_ref, layer_ref, fold_ref, work_ref, do_ref, delta_ref, dkv_ref, dqkv_ref, da1_ref, own_ref, passing_ref, passlayer_ref, bqv_ref,
    folded_ref, cross1_ref, far1_ref, mid1_ref, last1_ref, side1_ref,
    cross2_ref, far2_ref, mid2_ref, last2_ref, side2_ref,
    stagew_ref, landw_ref, workw_ref, crossw_ref, farw_ref, midw_ref, lastw_ref, sidew_ref,
    stage0_ref, land0_ref, work0_ref, cross0_ref, far0_ref, mid0_ref, last0_ref, side0_ref,
    sums_ref, sumland_ref,
    send_sem, recv_sem, local_sem, result_sem, group_sem,
):
    t = pl.program_id(0)
    n = own_ref.shape[0]
    width = gw_ref.shape[-1]
    depth = part0_ref.shape[0]
    heads = width // HEAD_DIM
    step = n // 4
    place = Place()
    y = place.y
    links = Links(send_sem, recv_sem)
    k, i = group_and_block(t)
    mine = place.group(k)
    now = k % 2
    out = Result(links, place, own_ref, passing_ref, out_ref, step // 2, result_sem.at[0], 8)
    layer = Result(links, place, layer_ref, passlayer_ref, layerout_ref, step, result_sem.at[1], 3)
    fetch = pltpu.make_async_copy(tokens_ref.at[place.t], own_ref, local_sem.at[0])
    fetch_layer, fetch_work, fetch_fold, fetch_gbt, fetch_a1t = [
        pltpu.make_async_copy(there, here, local_sem.at[1 + j])
        for j, (there, here) in enumerate([
            (layer_in, layer_ref), (work_in, work_ref), (fold_in, fold_ref),
            (gbt_in, gbt_ref), (a1t_in, a1t_ref),
        ])
    ]
    def operands(group):
        slot = group % 2
        pairs = [
            (gw_in, gw_ref), (scale_in, scale_ref), (o_in, o_ref), (v_in, v_ref),
            (q_in, q_ref), (kt_in, kt_ref), (gq_in, gq_ref),
        ]
        return [
            pltpu.make_async_copy(there.at[group], here.at[slot], group_sem.at[slot, j])
            for j, (there, here) in enumerate(pairs)
        ]

    corew = [links.add(place.to_core, stagew_ref, landw_ref.at[i], Z_DEV) for i in range(2)]
    core0 = [links.add(place.to_core, stage0_ref, land0_ref.at[i], Z_DEV) for i in range(2)]
    def half_done(i, *landing):
        return Reduce(
            links, place, lambda s, z, y: work_ref.at[i, z, y],
            lambda s, z: folded_ref.at[i, z] if s else fold_ref.at[i, z],
            *landing, slots=(1,),
        )

    seg1 = half_done(0, cross1_ref, far1_ref, mid1_ref, last1_ref, side1_ref)
    seg2 = half_done(1, cross2_ref, far2_ref, mid2_ref, last2_ref, side2_ref)
    segw = Reduce(
        links, place, lambda s, z, y: workw_ref.at[s, z, y],
        lambda s, z: workw_ref.at[s, z, y],
        crossw_ref, farw_ref, midw_ref, lastw_ref, sidew_ref,
    )
    seg0 = Reduce(
        links, place, lambda s, z, y: work0_ref.at[s, z, y],
        lambda s, z: work0_ref.at[s, z, y],
        cross0_ref, far0_ref, mid0_ref, last0_ref, side0_ref,
    )
    sum_core, sum_y, *sum_z, sum_x = [
        links.add(to, sums_ref.at[i], sumland_ref.at[j])
        for j, (i, to) in enumerate(
            zip([0, 1, 2, 2, 2, 3], [place.to_core, place.to_y] + place.to_z[1:] + [place.to_x])
        )
    ]

    def when(point):
        return pl.when(t == point)

    @when(0)
    def _():
        start(fetch_layer, operands(1), fetch_work, fetch_fold, fetch_gbt, operands(0))
        start(fetch, fetch_a1t)
        place.greet()
        fetch_layer.wait()
        for i in range(3):
            layer.send(i)
        fetch_work.wait()
        start(seg1.y[1], seg2.y[1])
        fetch_fold.wait()
        start(seg1.z[0][:2], seg2.z[0][:2])
        bqv_ref[...] = jnp.zeros_like(bqv_ref)
        sums_ref[0] = early_ref[...]
        fetch_gbt.wait()

    def add_core():
        recv(corew[1])

        @pl.loop(0, Z_DEV)
        def _(z):
            workw_ref[1, z] = (
                workw_ref[1, z].astype(F32) + landw_ref[1, z].astype(F32)
            ).astype(BF16)

        start(segw.y[1])

    def wait(copies):
        for copy in copies:
            copy.wait()

    @when(0)
    def _():
        wait(operands(1))

    @when(4)
    def _():
        start(operands(3))
        wait(operands(0))

    @when(8)
    def _():
        start(operands(2))
        wait(operands(3))

    @when(9)
    def _():
        wait(operands(2))

    plan = [
        (2, 1, lambda: (seg1.fold_y(1, 0), seg1.fold_z(0))),
        (3, 1, lambda: layer.pass_on(0)),
        (4, 0, lambda: (seg1.fold_y(1, 1), seg2.fold_z(0))),
        (4, 1, lambda: layer.pass_on(1)),
        (5, 1, lambda: (seg1.fold_z(1), seg2.fold_y(1, 0))),
        (8, 0, lambda: (seg2.fold_y(1, 1), layer.pass_on(2))),
        (8, 1, lambda: (seg1.send_x(), segw.fold_y(0, 0), segw.fold_y(0, 1))),
        (9, 0, add_core),
        (9, 1, lambda: (seg2.fold_z(1), seg0.fold_y(0, 0))),
        (10, 1, lambda: segw.fold_z(0)),
        (11, 1, lambda: (seg2.send_x(), seg0.fold_y(0, 1))),
        (12, 1, lambda: (segw.fold_y(1, 0), segw.fold_y(1, 1))),
        (13, 1, lambda: (seg0.fold_z(0), (out.pass_on(7), out.pass_on(6)))),
        (14, 1, lambda: segw.fold_z(1)),
    ]

    def serve(point):
        for at, where, act in plan:
            if where == point:
                pl.when(t == at)(lambda act=act: (act(), None)[1])

    @pl.when((t == 0) | (t == 4) | (t == 8) | (t == 9))
    def _():
        pick = (
            lax.broadcasted_iota(jnp.int32, (8, width), 1) // HEAD_DIM
            == lax.broadcasted_iota(jnp.int32, (8, width), 0)
        ).astype(BF16)

        @pl.loop(0, n // step)
        def _(i):
            rows = pl.ds(pl.multiple_of(i * step, step), step)
            columns = scale_ref[now, :, rows].T
            lane = lax.broadcasted_iota(jnp.int32, (step, width), 1)
            scale = columns[:, heads - 1 : heads]
            for h in reversed(range(heads - 1)):
                scale = jnp.where(lane < (h + 1) * HEAD_DIM, columns[:, h : h + 1], scale)
            do = (dot_nn(gb_ref[rows, :], gw_ref[now]) * scale).astype(BF16)
            do_ref[now, rows, :] = do
            product = do.astype(F32) * o_ref[now, rows, :].astype(F32)
            high = product.astype(BF16)
            low = (product - high.astype(F32)).astype(BF16)
            delta_ref[now, :, rows] = dot_nt(pick, high) + dot_nt(pick, low)

        value = dot_nn(gbt_ref[...], o_ref[now]).reshape(Z_DEV, Y_DEV, depth, width)
        for s in range(2):
            @when(8 * s)
            def _():
                if s:
                    corew[0].wait_send()
                stagew_ref[...] = value.astype(BF16)
                start(corew[s])

        @when(4)
        def _():
            recv(corew[0])
            workw_ref[0] = (value + landw_ref[0].astype(F32)).astype(BF16)
            start(segw.y[0])

        @when(9)
        def _():
            workw_ref[1] = value.astype(BF16)

    serve(0)

    for ii in reversed(range(4)):
        @pl.when(i == ii)
        def _():
            first, last = ii * step, (ii + 1) * step
            do = do_ref[now, first:last, :]
            q = q_ref[now, first:last, :]
            v = v_ref[now, :last, :]
            lane = lax.broadcasted_iota(jnp.int32, (1, width), 1)
            dk, dv, dq = None, None, []
            for h in range(heads):
                low, high = h * HEAD_DIM, (h + 1) * HEAD_DIM
                here = (lane >= low) & (lane < high)
                p = p_ref[0, h, 0, :last, :]
                dp = dot_nt(v, jnp.where(here, do, jnp.zeros((), BF16)))
                ds = p * (dp - delta_ref[now, h : h + 1, first:last]).astype(BF16)
                part = dot_nn(p, do)
                dv = part if dv is None else jnp.where(lane < low, dv, part)
                part = dot_nn(ds, q)
                dk = part if dk is None else jnp.where(lane < low, dk, part)
                dq.append(dot_nn(kt_ref[now, low:high, :last], ds))
            if ii == 3:
                dkv_ref[now, 0] = dk
                dkv_ref[now, 1] = dv
            else:
                dkv_ref[now, 0, :last, :] += dk
                dkv_ref[now, 1, :last, :] += dv
            dk = dkv_ref[now, 0, first:last, :].astype(BF16)
            dv = dkv_ref[now, 1, first:last, :].astype(BF16)
            dq = (jnp.concatenate(dq, 0) * HEAD_DIM ** -0.5).astype(BF16).T
            dqkv_ref[now, first:last, :width] = dq
            dqkv_ref[now, first:last, width : 2 * width] = dk
            dqkv_ref[now, first:last, 2 * width :] = dv
            bqv_ref[mine, 0:1, :] += jnp.sum(dq.astype(F32), 0, keepdims=True)
            bqv_ref[mine, 1:2, :] += jnp.sum(dv.astype(F32), 0, keepdims=True)

            @pl.when(t >= 8)
            def _():
                da1_ref[first:last, :] += dot_nt(dqkv_ref[now, first:last, :], gq_ref[now])

    serve(1)

    @pl.when((t > 8) & (t % 2 == 1))
    def _():
        rows = pl.ds(pl.multiple_of(i * step, step), step)
        xhat, r = norm_parts(own_ref[rows, :].astype(F32))
        da1 = da1_ref[rows, :]
        sums_ref[0, 0:1, :] += jnp.sum(da1 * xhat, 0, keepdims=True)
        sums_ref[0, 2:3, :] += jnp.sum(da1, 0, keepdims=True)
        dg = da1 * rows_ref[0:1, :]
        dv = r * (
            dg
            - jnp.mean(dg, -1, keepdims=True)
            - xhat * jnp.mean(dg * xhat, -1, keepdims=True)
        )
        own_ref[rows, :] = (dh1_ref[...] + dv).astype(BF16)
        for ii in range(4):
            @pl.when(i == ii)
            def _():
                out.send(2 * ii + 1)
                out.send(2 * ii)

    @pl.when((t == 3) | (t == 7) | (t > 13))
    def _():
        @when(3)
        def _():
            fetch.wait()
            fetch_a1t.wait()

        @when(3)
        def _():
            da1_ref[...] = dot_nt(dqkv_ref[now], gq_ref[now])

        @when(7)
        def _():
            da1_ref[...] += dot_nt(dqkv_ref[now], gq_ref[now])

        value = dot_nn(a1t_ref[...], dqkv_ref[now]).reshape(Z_DEV, Y_DEV, depth, 3 * width)
        for s in range(2):
            @when(3 + 11 * s)
            def _():
                if s:
                    core0[0].wait_send()
                stage0_ref[...] = value.astype(BF16)
                start(core0[s])

            @when(7 + 8 * s)
            def _():
                recv(core0[s])
                work0_ref[s] = (value + land0_ref[s].astype(F32)).astype(BF16)
                start(seg0.y[s])

    @when(15)
    def _():
        for s in range(4):
            sums_ref[0, 3:5, s * width : (s + 1) * width] = bqv_ref[s, 0:2, :]
        start(sum_core)
        segw.send_x()
        out.pass_on(5)
        out.pass_on(4)
        recv(sum_core)
        sums_ref[1] = sums_ref[0] + sumland_ref[0]
        start(sum_y)
        seg0.fold_y(1, 0)
        out.pass_on(3)
        out.pass_on(2)
        seg0.fold_y(1, 1)
        recv(sum_y)
        sums_ref[2] = sums_ref[1] + sumland_ref[1]
        start(sum_z)
        seg0.fold_z(1)
        recv(sum_z)
        sums_ref[3] = (sums_ref[2] + sumland_ref[2]) + (sumland_ref[3] + sumland_ref[4])
        start(sum_x)
        part1_ref[...] = seg1.total()
        part2_ref[...] = seg2.total()
        seg0.send_x()
        partw_ref[...] = segw.total()
        layer.finish()
        out.pass_on(1)
        out.pass_on(0)
        recv(sum_x)
        total_ref[...] = sums_ref[3] + sumland_ref[5]
        part0_ref[...] = seg0.total()
        out.finish()
        links.sent(corew[0], core0[0])


def group_and_block(t):
    early = t < 8
    return (
        jnp.where(early, 1 - t // 4, 3 - t % 2),
        3 - jnp.where(early, t % 4, jnp.maximum(t - 8, 0) // 2),
    )


def run_fused_backward(
    tokens, gq, gw, rows, dh1, gb, gbt, q, v, kt, p, scale, o, a1t, layer, fold, work, early
):
    groups, n, _ = tokens.shape
    width = gw.shape[-1]
    heads = width // HEAD_DIM
    hidden = fold.shape[-1]
    depth = D // (Z_DEV * Y_DEV)
    step = n // 4

    p_spec = pl.BlockSpec(
        (1, heads, 1, n, step),
        lambda t: (group_and_block(t)[0], 0, group_and_block(t)[1], 0, 0),
    )

    copies = 24 + 9 + 4 + 2 * 15 + 2 * 11 + 6

    def landing(lanes):
        return [
            pltpu.VMEM((2, Z_DEV, depth, lanes), BF16),
            pltpu.VMEM((2, 3, depth, lanes), BF16), pltpu.VMEM((2, 2, depth, lanes), BF16),
            pltpu.VMEM((depth, lanes), BF16), pltpu.VMEM((depth, lanes), BF16),
        ]

    def working(lanes):
        block = (Z_DEV, Y_DEV, depth, lanes)
        return [pltpu.VMEM(block, BF16)] + [pltpu.VMEM((2,) + block, BF16)] * 2

    return pl.pallas_call(
        fused_backward,
        grid=(4 * groups,),
        in_specs=[
            ANY_WHOLE, ANY_WHOLE, ANY_WHOLE, VMEM_WHOLE,
            pl.BlockSpec((step, D), lambda t: (group_and_block(jnp.maximum(t, 8))[1], 0)),
            VMEM_WHOLE, ANY_WHOLE, ANY_WHOLE, ANY_WHOLE, ANY_WHOLE, p_spec,
            ANY_WHOLE, ANY_WHOLE, ANY_WHOLE, ANY_WHOLE, ANY_WHOLE, ANY_WHOLE, VMEM_WHOLE,
        ],
        out_specs=[ANY_WHOLE] * 2 + [VMEM_WHOLE] * 5,
        out_shape=[
            shaped(BF16, groups, n, D), shaped(BF16, groups, n - step, D),
            shaped(F32, depth, 3 * width),
            shaped(F32, depth, width), shaped(F32, depth, hidden),
            shaped(F32, depth, hidden), shaped(F32, 16, D),
        ],
        scratch_shapes=[
            pltpu.VMEM((2, D, 3 * width), BF16), pltpu.VMEM((2, D, width), BF16),
            pltpu.VMEM((2, n, width), BF16), pltpu.VMEM((2, n, width), BF16),
            pltpu.VMEM((2, width, n), BF16), pltpu.VMEM((2, 8, n), F32),
            pltpu.VMEM((2, n, width), BF16),
            pltpu.VMEM((D, n), BF16), pltpu.VMEM((D, n), BF16), pltpu.VMEM((n - step, D), BF16),
            pltpu.VMEM((2, Z_DEV, depth, hidden), BF16),
            pltpu.VMEM((2, Z_DEV, Y_DEV, depth, hidden), BF16),
            pltpu.VMEM((2, n, width), BF16),
            pltpu.VMEM((2, 8, n), F32), pltpu.VMEM((2, 2, n, width), F32),
            pltpu.VMEM((2, n, 3 * width), BF16), pltpu.VMEM((n, D), F32),
            pltpu.VMEM((n, D), BF16), pltpu.VMEM((n, D), BF16), pltpu.VMEM((n - step, D), BF16),
            pltpu.VMEM((groups, 8, width), F32),
        ]
        + landing(hidden)[:1] + landing(hidden) + landing(hidden)
        + working(width) + landing(width)
        + working(3 * width) + landing(3 * width)
        + [
            pltpu.VMEM((4, 16, D), F32), pltpu.VMEM((6, 16, D), F32),
            pltpu.SemaphoreType.DMA((copies,)), pltpu.SemaphoreType.DMA((copies,)),
            pltpu.SemaphoreType.DMA((6,)), pltpu.SemaphoreType.DMA((2, 2, 8)),
            pltpu.SemaphoreType.DMA((2, 7)),
        ],
        compiler_params=pltpu.CompilerParams(
            vmem_limit_bytes=VMEM_LIMIT, collective_id=2, has_side_effects=True
        ),
        name="fused_backward",
    )(tokens, gq, gw, rows, dh1, gb, gbt, q, v, kt, p, scale, o, a1t, layer, fold, work, early)


def place_gradients(
    tie_ref, sums_ref, part0_ref, partw_ref, part1_ref, part2_ref, near_out_ref, near_rest_ref,
    near_grad_ref, far_out_ref, far_grad_ref, gains_ref, bias_ref, in_ref, out_ref, expand_ref,
    project_ref,
):
    first = near_out_ref.shape[1]
    far_out_ref[0, :first] = near_out_ref[0]
    far_out_ref[0, first:] = near_rest_ref[0]
    far_grad_ref[...] = near_grad_ref[...]
    own = gains_ref.shape[-1]
    width = partw_ref.shape[-1]

    @pl.when(pl.program_id(0) == 0)
    def _():
        origin = (lax.axis_index("dp") * 4 + lax.axis_index("tensor")) * own
        feature = lax.broadcasted_iota(jnp.int32, (D, 128), 0)
        lane = lax.broadcasted_iota(jnp.int32, (D, 128), 1)
        chosen = ((feature == origin + lane) & (lane < own)).astype(F32)
        sums = lax.dot_general(
            sums_ref[...], chosen, (((1,), (0,)), ((), ())),
            precision=lax.Precision.HIGHEST, preferred_element_type=F32,
        )[:, :own]
        s0, s1, s2, s3 = tie_ref[0], tie_ref[1], tie_ref[2], tie_ref[3]
        w_out = partw_ref[...].T

        def at(source, wanted, value):
            return jnp.where(source == wanted, value, jnp.zeros_like(value))

        row = lax.broadcasted_iota(jnp.int32, (NSRC, own), 0)
        for i, wanted in enumerate([s0, s0, s0, s1, s2, s3, s2, s2, s2, s2]):
            bias_ref[i] = jnp.where(row == wanted, sums[2 + i : 3 + i], 0.0)
        for s in range(NSRC):
            gains_ref[s, 0:1] = at(s, s0, sums[0:1])
            gains_ref[s, 1:2] = at(s, s2, sums[1:2])
            for j in range(3):
                in_ref[s, j] = at(s, s0, part0_ref[:, j * width : (j + 1) * width])
            out_ref[s] = at(s, s1, w_out)
            expand_ref[s] = at(s, s2, part1_ref[...])
            project_ref[s] = at(s, s3, part2_ref[...])


def run_place_gradients(tie, sums, part0, partw, part1, part2, out, rest, grad, like):
    slots, n, _ = grad.shape
    gains, biases, w_in, w_out, w_expand, w_project = [item.shape for item in like]
    shapes = [
        gains, (biases[1], biases[0], biases[2]), w_in, w_out, w_expand,
        (w_project[0], w_project[2], w_project[1]),
    ]
    out, grad, gains, biases, w_in, w_out, w_expand, w_project = pl.pallas_call(
        place_gradients,
        grid=(slots,),
        in_specs=[SMEM_WHOLE] + [VMEM_WHOLE] * 5
        + [group(n // 4, D), group(n - n // 4, D), group(n, D)],
        out_specs=[group(n, D), group(n, D)] + [VMEM_WHOLE] * 6,
        out_shape=[shaped(BF16, slots, n, D)] * 2 + [shaped(F32, *item) for item in shapes],
        compiler_params=pltpu.CompilerParams(vmem_limit_bytes=VMEM_LIMIT),
        name="place_gradients",
    )(tie, sums, part0, partw, part1, part2, out, rest, grad)
    biases = biases.transpose(1, 0, 2)
    return out, grad, gains, biases, w_in, w_out, w_expand, w_project.transpose(0, 2, 1)


def plain_step(
    tokens, lengths, tie_map, norm_gains, bias_rows, attention_in, attention_out,
    expand_weight, project_weight, cotangent,
):
    slot_rows = tokens.shape[0] // lengths.shape[0]
    me = lax.axis_index("tensor")
    in_local = lax.dynamic_index_in_dim(attention_in, tie_map[0], 0, keepdims=False)
    out_local = lax.dynamic_index_in_dim(attention_out, tie_map[1], 0, keepdims=False)
    expand_local = lax.dynamic_index_in_dim(expand_weight, tie_map[2], 0, keepdims=False)
    project_local = lax.dynamic_index_in_dim(project_weight, tie_map[3], 0, keepdims=False)
    local0 = jnp.concatenate([in_local, out_local.T[None]], 0)
    row_kinds = jnp.array([0, 0, 0, 1, 2, 3] + [2] * (FF // D), dtype=jnp.int32)
    gain_kinds = jnp.array([0, 2], dtype=jnp.int32)
    gain_pick = norm_gains[tie_map[gain_kinds], jnp.arange(2)]
    bias_pick = bias_rows[tie_map[row_kinds], jnp.arange(row_kinds.shape[0])]
    vectors = jnp.concatenate([gain_pick, bias_pick], 0)
    x = lax.dynamic_slice_in_dim(tokens, me * slot_rows, slot_rows, 0)
    cot = lax.dynamic_slice_in_dim(cotangent, me * slot_rows, slot_rows, 0)
    length = lax.dynamic_slice_in_dim(lengths, me, 1, 0)
    rows = lax.all_gather(vectors, ("dp", "tensor"), axis=1, tiled=True).astype(F32)
    rows = jnp.concatenate([rows, jnp.zeros((4, D), F32)], 0)

    def gathered(piece, axis):
        piece = lax.all_gather(piece, "dp", axis=axis, tiled=True)
        return lax.all_gather(piece, "tensor", axis=0)

    g0 = gathered(local0, 1)
    g1 = gathered(expand_local, 0)
    g2 = gathered(project_local.T, 0)
    groups, width = g0.shape[0], g0.shape[-1]
    bqv = rows[3:5].reshape(2, groups, width).transpose(1, 0, 2)
    q, v, kt, p, o, a1t, h1, a2, a2t = run_attention_forward(length, x, g0, rows, bqv)
    out, d1, d2, dh1, gb, gbt, sums = run_feed_forward(length, cot, a2, a2t, h1, g1, g2, rows)
    d0, xg, sums_in, sums_qv = run_attention_backward(
        x, g0, rows, dh1, gb, gbt, q, v, kt, p, o, a1t
    )
    layer_out = lax.all_gather(out, "tensor", axis=0, tiled=True)
    tokens_grad = lax.all_gather(xg, "tensor", axis=0, tiled=True)

    def scattered(piece, axis):
        piece = lax.psum_scatter(piece, "tensor", scatter_dimension=0)
        return lax.psum_scatter(piece, "dp", scatter_dimension=axis, tiled=True).astype(F32)

    part0 = scattered(d0, 1)
    part1 = scattered(d1, 0)
    part2 = scattered(d2, 0)
    qv = sums_qv[:, :2].transpose(1, 0, 2).reshape(2, D)
    sums = jnp.concatenate(
        [sums_in[0:1], sums[1:2], sums_in[1:2], qv, sums[5:12]], 0
    )
    sums = lax.psum_scatter(sums, ("dp", "tensor"), scatter_dimension=1, tiled=True)
    return layer_out, tokens_grad, *placed(tie_map, sums, part0, part1, part2)


def fused_step(
    tokens, lengths, tie_map, norm_gains, bias_rows, attention_in, attention_out,
    expand_weight, project_weight, cotangent,
):
    slots = lengths.shape[0]
    tokens = tokens.reshape(slots, -1, D)
    cotangent = cotangent.reshape(slots, -1, D)
    gq, gw, g1, g2, rows, q, v, kt, p, scale, o, a1t, h1, a2, a2t = run_fused_forward(
        tie_map, lengths, tokens, norm_gains, bias_rows, attention_in, attention_out,
        expand_weight, project_weight,
    )
    out, layer, fold, work, dh1, gb, gbt, early = run_fused_feed_forward(
        lengths, cotangent, a2, a2t, h1, g1, g2, rows
    )
    grad, rest, part0, partw, part1, part2, sums = run_fused_backward(
        tokens, gq, gw, rows, dh1, gb, gbt, q, v, kt, p, scale, o, a1t, layer, fold,
        work, early,
    )
    out, grad, *placed_grads = run_place_gradients(
        tie_map, sums, part0, partw, part1, part2, out, rest, grad,
        (norm_gains, bias_rows, attention_in, attention_out, expand_weight, project_weight),
    )
    return out.reshape(-1, D), grad.reshape(-1, D), *placed_grads


def placed(tie_map, sums, part0, part1, part2):
    source = jnp.arange(NSRC, dtype=jnp.int32)

    def place(piece, which):
        pick = (source == tie_map[which]).reshape((NSRC,) + (1,) * piece.ndim)
        return jnp.where(pick, piece[None], 0.0)

    def place_rows(piece, kinds):
        pick = source[:, None] == tie_map[jnp.array(kinds, dtype=jnp.int32)][None, :]
        return jnp.where(pick[:, :, None], piece[None], 0.0)

    return (
        place_rows(sums[:2], [0, 2]),
        place_rows(sums[2:], [0, 0, 0, 1, 2, 3] + [2] * (FF // D)),
        place(part0[:3], 0),
        place(part0[3].T, 1),
        place(part1, 2),
        place(part2.T, 3),
    )


def solution(mesh):
    fused = mesh.shape["dp"] == Z_DEV * Y_DEV and mesh.shape["tensor"] == X_DEV * C_DEV
    return jax.shard_map(
        fused_step if fused else plain_step,
        mesh=mesh,
        in_specs=(
            P("dp", None),
            P("dp"),
            P(),
            P(None, None, ("dp", "tensor")),
            P(None, None, ("dp", "tensor")),
            P(None, None, "dp", "tensor"),
            P(None, "tensor", "dp"),
            P(None, "dp", "tensor"),
            P(None, "tensor", "dp"),
            P("dp", None),
        ),
        out_specs=(
            P("dp", None),
            P("dp", None),
            P(None, None, ("dp", "tensor")),
            P(None, None, ("dp", "tensor")),
            P(None, None, "dp", "tensor"),
            P(None, "tensor", "dp"),
            P(None, "dp", "tensor"),
            P(None, "tensor", "dp"),
        ),
        check_vma=False,
    )
```

```python
import jax
import jax.numpy as jnp
from jax import lax
from jax.experimental import pallas as pl
from jax.experimental.pallas import tpu as pltpu
from jax.sharding import PartitionSpec as P

D = 768
HEAD_DIM = 64
FF = 3072
NSRC = 4
EPS = 1e-05
MASKED = -1e30
F32 = jnp.float32
BF16 = jnp.bfloat16
VMEM_LIMIT = 60 * 1024 * 1024


def dot_nn(a, b):
    return lax.dot_general(a, b, (((1,), (0,)), ((), ())), preferred_element_type=F32)


def dot_nt(a, b):
    return lax.dot_general(a, b, (((1,), (1,)), ((), ())), preferred_element_type=F32)


def norm_parts(v):
    center = jnp.mean(v, -1, keepdims=True)
    centered = v - center
    r = lax.rsqrt(jnp.mean(centered * centered, -1, keepdims=True) + EPS)
    return centered * r, r


def head_mask(shape, h):
    lane = lax.broadcasted_iota(jnp.int32, shape, 1)
    return (lane >= h * HEAD_DIM) & (lane < (h + 1) * HEAD_DIM)


def blocks(total, size):
    return [slice(i * size, (i + 1) * size) for i in range(total // size)]


def attention_forward(
    len_ref, x_ref, g_ref, rows_ref, bqv_ref,
    q_ref, v_ref, kt_ref, p_ref, o_ref, a1t_ref, h1_ref, a2_ref, a2t_ref,
    a1_ref, k_ref, vt_ref, ot_ref, attn_ref,
):
    t = pl.program_id(0)
    n = x_ref.shape[0]
    width = g_ref.shape[-1]
    heads = width // HEAD_DIM
    step = 256
    length = len_ref[0]

    @pl.when(t == 0)
    def _():
        @pl.loop(0, n // step)
        def _(b):
            rows = pl.ds(pl.multiple_of(b * step, step), step)
            xhat, _ = norm_parts(x_ref[rows, :].astype(F32))
            a1 = xhat * rows_ref[0:1, :] + rows_ref[2:3, :]
            a1_ref[rows, :] = a1.astype(BF16)
            a1t_ref[:, rows] = a1.astype(BF16).T
            attn_ref[rows, :] = x_ref[rows, :].astype(F32) + rows_ref[5:6, :]

    @pl.loop(0, n // step)
    def _(b):
        rows = pl.ds(pl.multiple_of(b * step, step), step)
        a1 = a1_ref[rows, :]
        q = (dot_nn(a1, g_ref[0, 0]) + bqv_ref[0, 0:1, :]).astype(BF16)
        q_ref[0, rows, :] = q * jnp.asarray(HEAD_DIM ** -0.5, BF16)
        k = dot_nn(a1, g_ref[0, 1]).astype(BF16)
        k_ref[rows, :] = k
        kt_ref[0, :, rows] = k.T
        v = (dot_nn(a1, g_ref[0, 2]) + bqv_ref[0, 1:2, :]).astype(BF16)
        v_ref[0, rows, :] = v
        vt_ref[:, rows] = v.T

    for h in range(heads):
        k = k_ref[...]
        k = jnp.where(head_mask(k.shape, h), k, jnp.zeros_like(k))
        for b in range(n // step):
            first, last = b * step, (b + 1) * step
            q = q_ref[0, first:last, :]
            key = lax.broadcasted_iota(jnp.int32, (last, step), 0)
            query = lax.broadcasted_iota(jnp.int32, (step, step), 1) + first
            s = dot_nt(k[:last], q)
            near = jnp.where(
                (key[first:] <= query) & (key[first:] < length), s[first:], MASKED
            )
            if b:
                far = jnp.where(key[:first] < length, s[:first], MASKED)
                top = jnp.maximum(
                    jnp.max(far, 0, keepdims=True), jnp.max(near, 0, keepdims=True)
                )
                e_far = jnp.exp(far - top)
                e_near = jnp.exp(near - top)
                total = jnp.sum(e_far, 0, keepdims=True) + jnp.sum(e_near, 0, keepdims=True)
                scale = 1.0 / total
                p_ref[0, h, :first, first:last] = (e_far * scale).astype(BF16)
            else:
                top = jnp.max(near, 0, keepdims=True)
                e_near = jnp.exp(near - top)
                scale = 1.0 / jnp.sum(e_near, 0, keepdims=True)
            p_ref[0, h, first:last, first:last] = (e_near * scale).astype(BF16)
            ot_ref[h * HEAD_DIM : (h + 1) * HEAD_DIM, first:last] = dot_nn(
                vt_ref[h * HEAD_DIM : (h + 1) * HEAD_DIM, :last],
                p_ref[0, h, :last, first:last],
            ).astype(BF16)

    @pl.loop(0, n // step)
    def _(b):
        rows = pl.ds(pl.multiple_of(b * step, step), step)
        o = ot_ref[:, rows].T
        o_ref[0, rows, :] = o
        attn_ref[rows, :] += dot_nt(o, g_ref[0, 3])

    @pl.when(t == pl.num_programs(0) - 1)
    def _():
        @pl.loop(0, n // step)
        def _(b):
            rows = pl.ds(pl.multiple_of(b * step, step), step)
            h1 = attn_ref[rows, :]
            h1_ref[rows, :] = h1
            xhat, _ = norm_parts(h1)
            a2 = (xhat * rows_ref[1:2, :] + rows_ref[6:7, :]).astype(BF16)
            a2_ref[rows, :] = a2
            a2t_ref[:, rows] = a2.T


SQRT_2_PI = 0.7978845608028654


def feed_forward_both(
    len_ref, c_ref, a2_ref, a2t_ref, h1_ref, w1_ref, w2_ref, rows_ref,
    out_ref, d1_ref, d2_ref, dh1_ref, gb_ref, gbt_ref, sums_ref,
    gf_ref, gft_ref, feed_ref, da2_ref, h_ref, df_ref,
):
    t = pl.program_id(0)
    n = c_ref.shape[0]
    step = 256
    length = len_ref[0]

    @pl.when(t == 0)
    def _():
        sums_ref[...] = jnp.zeros_like(sums_ref)

        @pl.loop(0, n // step)
        def _(b):
            rows = pl.ds(pl.multiple_of(b * step, step), step)
            place = b * step + lax.broadcasted_iota(jnp.int32, (step, 1), 0)
            live = (place < length).astype(F32)
            g = (c_ref[rows, :].astype(F32) * live).astype(BF16)
            gf_ref[rows, :] = g
            gft_ref[:, rows] = g.T
            sums_ref[7:8, :] += jnp.sum(g.astype(F32), 0, keepdims=True)

    bias = rows_ref[pl.ds(8 + t, 1), :]

    @pl.loop(0, n // step)
    def _(b):
        rows = pl.ds(pl.multiple_of(b * step, step), step)
        f = dot_nn(a2_ref[rows, :], w1_ref[0]) + bias
        dh = dot_nn(gf_ref[rows, :], w2_ref[0])
        f2 = f * f
        th = jnp.tanh(f * (SQRT_2_PI + (SQRT_2_PI * 0.044715) * f2))
        half = 0.5 + 0.5 * th
        h = (f * half).astype(BF16)
        slope = half + f * (0.5 - 0.5 * th * th) * (
            SQRT_2_PI + (3 * SQRT_2_PI * 0.044715) * f2
        )
        df = (dh * slope).astype(BF16)
        h_ref[rows, :] = h
        df_ref[rows, :] = df
        sums_ref[pl.ds(8 + t, 1), :] += jnp.sum(df.astype(F32), 0, keepdims=True)
        feed = dot_nt(h, w2_ref[0])
        da2 = dot_nt(df, w1_ref[0])

        @pl.when(t == 0)
        def _():
            feed_ref[rows, :] = feed
            da2_ref[rows, :] = da2

        @pl.when(t > 0)
        def _():
            feed_ref[rows, :] += feed
            da2_ref[rows, :] += da2

    @pl.loop(0, D // step)
    def _(b):
        rows = pl.ds(pl.multiple_of(b * step, step), step)
        d1_ref[0, rows, :] = dot_nn(a2t_ref[rows, :], df_ref[...]).astype(BF16)
        d2_ref[0, rows, :] = dot_nn(gft_ref[rows, :], h_ref[...]).astype(BF16)

    @pl.when(t == pl.num_programs(0) - 1)
    def _():
        @pl.loop(0, n // step)
        def _(b):
            rows = pl.ds(pl.multiple_of(b * step, step), step)
            place = b * step + lax.broadcasted_iota(jnp.int32, (step, 1), 0)
            live = (place < length).astype(F32)
            h1 = h1_ref[rows, :]
            out_ref[rows, :] = (live * (h1 + (feed_ref[rows, :] + rows_ref[7:8, :]))).astype(BF16)
            xhat, r = norm_parts(h1)
            da2 = da2_ref[rows, :]
            sums_ref[1:2, :] += jnp.sum(da2 * xhat, 0, keepdims=True)
            sums_ref[6:7, :] += jnp.sum(da2, 0, keepdims=True)
            dg = da2 * rows_ref[1:2, :]
            dv = r * (
                dg
                - jnp.mean(dg, -1, keepdims=True)
                - xhat * jnp.mean(dg * xhat, -1, keepdims=True)
            )
            dh1 = live * c_ref[rows, :].astype(F32) + dv
            dh1_ref[rows, :] = dh1
            gb = dh1.astype(BF16)
            gb_ref[rows, :] = gb
            gbt_ref[:, rows] = gb.T
            sums_ref[5:6, :] += jnp.sum(gb.astype(F32), 0, keepdims=True)


def attention_backward(
    x_ref, g_ref, rows_ref, dh1_ref, gb_ref, gbt_ref, q_ref, v_ref, kt_ref, p_ref,
    o_ref, a1t_ref,
    d0_ref, xg_ref, sums_ref, bqv_ref,
    do_ref, delta_ref, dqt_ref, dq_ref, dk_ref, dv_ref, da1_ref,
):
    t = pl.program_id(0)
    n = x_ref.shape[0]
    width = g_ref.shape[-1]
    heads = width // HEAD_DIM
    step = 256
    pick = (
        lax.broadcasted_iota(jnp.int32, (16, width), 1) // HEAD_DIM
        == lax.broadcasted_iota(jnp.int32, (16, width), 0)
    ).astype(BF16)

    @pl.loop(0, n // step)
    def _(b):
        rows = pl.ds(pl.multiple_of(b * step, step), step)
        do = dot_nn(gb_ref[rows, :], g_ref[0, 3]).astype(BF16)
        do_ref[rows, :] = do
        prod = do.astype(F32) * o_ref[0, rows, :].astype(F32)
        high = prod.astype(BF16)
        low = (prod - high.astype(F32)).astype(BF16)
        delta_ref[:, rows] = dot_nt(pick, high) + dot_nt(pick, low)

    dqt_ref[...] = jnp.zeros_like(dqt_ref)
    for b in range(n // step):
        first, last = b * step, (b + 1) * step
        do = do_ref[first:, :]
        q = q_ref[0, first:, :]
        v = v_ref[0, first:last, :]
        dk, dv = None, None
        for h in range(heads):
            mine = head_mask((1, width), h)
            zero = jnp.zeros((), BF16)
            p = p_ref[0, h, first:last, first:]
            dp = dot_nt(jnp.where(mine, v, zero), do)
            ds = (p.astype(F32) * (dp - delta_ref[h : h + 1, first:])).astype(BF16)
            part = dot_nn(p, jnp.where(mine, do, zero))
            dv = part if dv is None else dv + part
            part = dot_nn(ds, jnp.where(mine, q, zero))
            dk = part if dk is None else dk + part
            head = slice(h * HEAD_DIM, (h + 1) * HEAD_DIM)
            dqt_ref[head, first:] += dot_nn(kt_ref[0, head, first:last], ds)
        dk_ref[first:last, :] = dk.astype(BF16)
        dv_ref[first:last, :] = dv.astype(BF16)

    @pl.when(t == 0)
    def _():
        da1_ref[...] = jnp.zeros_like(da1_ref)

    bqv_ref[...] = jnp.zeros_like(bqv_ref)

    @pl.loop(0, n // step)
    def _(b):
        rows = pl.ds(pl.multiple_of(b * step, step), step)
        dq = (dqt_ref[:, rows] * HEAD_DIM ** -0.5).astype(BF16).T
        dk = dk_ref[rows, :]
        dv = dv_ref[rows, :]
        dq_ref[rows, :] = dq
        bqv_ref[0, 0:1, :] += jnp.sum(dq.astype(F32), 0, keepdims=True)
        bqv_ref[0, 1:2, :] += jnp.sum(dv.astype(F32), 0, keepdims=True)
        da1_ref[rows, :] += (
            dot_nt(dq, g_ref[0, 0]) + dot_nt(dk, g_ref[0, 1]) + dot_nt(dv, g_ref[0, 2])
        )

    @pl.loop(0, D // step)
    def _(b):
        rows = pl.ds(pl.multiple_of(b * step, step), step)
        a1t = a1t_ref[rows, :]
        d0_ref[0, 0, rows, :] = dot_nn(a1t, dq_ref[...]).astype(BF16)
        d0_ref[0, 1, rows, :] = dot_nn(a1t, dk_ref[...]).astype(BF16)
        d0_ref[0, 2, rows, :] = dot_nn(a1t, dv_ref[...]).astype(BF16)
        d0_ref[0, 3, rows, :] = dot_nn(gbt_ref[rows, :], o_ref[0]).astype(BF16)

    @pl.when(t == pl.num_programs(0) - 1)
    def _():
        sums_ref[...] = jnp.zeros_like(sums_ref)

        @pl.loop(0, n // step)
        def _(b):
            rows = pl.ds(pl.multiple_of(b * step, step), step)
            xhat, r = norm_parts(x_ref[rows, :].astype(F32))
            da1 = da1_ref[rows, :]
            sums_ref[0:1, :] += jnp.sum(da1 * xhat, 0, keepdims=True)
            sums_ref[1:2, :] += jnp.sum(da1, 0, keepdims=True)
            dg = da1 * rows_ref[0:1, :]
            dv = r * (
                dg
                - jnp.mean(dg, -1, keepdims=True)
                - xhat * jnp.mean(dg * xhat, -1, keepdims=True)
            )
            xg_ref[rows, :] = (dh1_ref[rows, :] + dv).astype(BF16)


def whole(*shape):
    return pl.BlockSpec(shape, lambda t: (0,) * len(shape))


def group(*shape):
    return pl.BlockSpec((1,) + shape, lambda t: (t,) + (0,) * len(shape))


def shaped(dtype, *shape):
    return jax.ShapeDtypeStruct(shape, dtype)


SMEM_WHOLE = pl.BlockSpec(memory_space=pltpu.SMEM)


def run_attention_forward(length, x, g0, rows, bqv):
    n = x.shape[0]
    groups, _, _, width = g0.shape
    heads = width // HEAD_DIM
    return pl.pallas_call(
        attention_forward,
        grid=(groups,),
        in_specs=[SMEM_WHOLE, whole(n, D), group(4, D, width), whole(16, D), group(2, width)],
        out_specs=[
            group(n, width), group(n, width), group(width, n), group(heads, n, n),
            group(n, width), whole(D, n), whole(n, D), whole(n, D), whole(D, n),
        ],
        out_shape=[
            shaped(BF16, groups, n, width), shaped(BF16, groups, n, width),
            shaped(BF16, groups, width, n), shaped(BF16, groups, heads, n, n),
            shaped(BF16, groups, n, width), shaped(BF16, D, n), shaped(F32, n, D),
            shaped(BF16, n, D), shaped(BF16, D, n),
        ],
        scratch_shapes=[
            pltpu.VMEM((n, D), BF16), pltpu.VMEM((n, width), BF16),
            pltpu.VMEM((width, n), BF16), pltpu.VMEM((width, n), BF16),
            pltpu.VMEM((n, D), F32),
        ],
        compiler_params=pltpu.CompilerParams(vmem_limit_bytes=VMEM_LIMIT),
        name="attention_forward",
    )(length, x, g0, rows, bqv)


def run_feed_forward(length, cot, a2, a2t, h1, g1, g2, rows):
    n = cot.shape[0]
    groups, _, width = g1.shape
    return pl.pallas_call(
        feed_forward_both,
        grid=(groups,),
        in_specs=[
            SMEM_WHOLE, whole(n, D), whole(n, D), whole(D, n), whole(n, D),
            group(D, width), group(D, width), whole(16, D),
        ],
        out_specs=[
            whole(n, D), group(D, width), group(D, width), whole(n, D), whole(n, D),
            whole(D, n), whole(16, D),
        ],
        out_shape=[
            shaped(BF16, n, D), shaped(BF16, groups, D, width), shaped(BF16, groups, D, width),
            shaped(F32, n, D), shaped(BF16, n, D), shaped(BF16, D, n), shaped(F32, 16, D),
        ],
        scratch_shapes=[
            pltpu.VMEM((n, D), BF16), pltpu.VMEM((D, n), BF16), pltpu.VMEM((n, D), F32),
            pltpu.VMEM((n, D), F32), pltpu.VMEM((n, width), BF16), pltpu.VMEM((n, width), BF16),
        ],
        compiler_params=pltpu.CompilerParams(vmem_limit_bytes=VMEM_LIMIT),
        name="feed_forward_both",
    )(length, cot, a2, a2t, h1, g1, g2, rows)


def run_attention_backward(x, g0, rows, dh1, gb, gbt, q, v, kt, p, o, a1t):
    n = x.shape[0]
    groups, _, _, width = g0.shape
    heads = width // HEAD_DIM
    return pl.pallas_call(
        attention_backward,
        grid=(groups,),
        in_specs=[
            whole(n, D), group(4, D, width), whole(16, D), whole(n, D), whole(n, D),
            whole(D, n), group(n, width), group(n, width), group(width, n),
            group(heads, n, n), group(n, width), whole(D, n),
        ],
        out_specs=[group(4, D, width), whole(n, D), whole(8, D), group(8, width)],
        out_shape=[
            shaped(BF16, groups, 4, D, width), shaped(BF16, n, D), shaped(F32, 8, D),
            shaped(F32, groups, 8, width),
        ],
        scratch_shapes=[
            pltpu.VMEM((n, width), BF16), pltpu.VMEM((16, n), F32), pltpu.VMEM((width, n), F32),
            pltpu.VMEM((n, width), BF16), pltpu.VMEM((n, width), BF16),
            pltpu.VMEM((n, width), BF16), pltpu.VMEM((n, D), F32),
        ],
        compiler_params=pltpu.CompilerParams(vmem_limit_bytes=VMEM_LIMIT),
        name="attention_backward",
    )(x, g0, rows, dh1, gb, gbt, q, v, kt, p, o, a1t)


Z_DEV, Y_DEV, X_DEV, C_DEV = 4, 2, 2, 2


class Place:
    def __init__(self):
        dp, self.t = lax.axis_index("dp"), lax.axis_index("tensor")
        self.dp = dp
        self.z, self.y = dp // 2, dp % 2
        self.x, self.c = self.t // 2, self.t % 2
        self.other_y = 1 - self.y
        self.zs = [
            self.z,
            self.z + 1 - 2 * (self.z % 2),
            self.z + 2 - 4 * (self.z // 2),
            3 - self.z,
        ]
        self.ts = [
            self.t,
            self.t + 1 - 2 * (self.t % 2),
            self.t + 2 - 4 * (self.t // 2),
            3 - self.t,
        ]
        self.to_z = [dict(dp=z * 2 + self.y) for z in self.zs]
        self.to_y = dict(dp=self.z * 2 + self.other_y)
        self.to_x = dict(tensor=self.ts[2])
        self.same_t = self.to_z[1:] + [dict(dp=z * 2 + self.other_y) for z in self.zs]
        self.same_dp = [dict(tensor=t) for t in self.ts[1:]]
        self.to_core = dict(tensor=self.ts[1])

    def group(self, k):
        return lax.select(
            k == 0, self.ts[0],
            lax.select(k == 1, self.ts[1], lax.select(k == 2, self.ts[2], self.ts[3])),
        )

    def greet(self, others=None):
        barrier = pltpu.get_barrier_semaphore()
        others = others or self.to_z[1:] + [self.to_y, self.to_x, self.to_core]
        for device in others:
            pl.semaphore_signal(
                barrier, inc=1, device_id=device, device_id_type=pl.DeviceIdType.MESH
            )
        pl.semaphore_wait(barrier, len(others))


class Pieces:
    def __init__(self, whole, pieces):
        self.whole, self.pieces = whole, pieces

    def start(self):
        for piece in self.pieces:
            piece.start()

    def wait_recv(self):
        self.whole.wait_recv()

    def wait_send(self):
        self.whole.wait_send()


class Links:
    def __init__(self, send_sem, recv_sem):
        self.send_sem, self.recv_sem = send_sem, recv_sem
        self.copies = []

    def add(self, device, src, dst, parts=1, axis=0):
        number = len(self.copies)

        def make(src, dst):
            return pltpu.make_async_remote_copy(
                src_ref=src,
                dst_ref=dst,
                send_sem=self.send_sem.at[number],
                recv_sem=self.recv_sem.at[number],
                device_id=device,
                device_id_type=pl.DeviceIdType.MESH,
            )

        size = src.shape[axis] // parts
        cuts = [(slice(None),) * axis + (pl.ds(i * size, size),) for i in range(parts)]
        copy = Pieces(make(src, dst), [make(src.at[cut], dst.at[cut]) for cut in cuts])
        self.copies.append(copy)
        return copy

    def sent(self, *apart):
        for copy in self.copies:
            if all(copy is not other for other in apart):
                copy.wait_send()


def flat(copies):
    for item in copies:
        if isinstance(item, list):
            yield from flat(item)
        else:
            yield item


def start(*copies):
    for copy in flat(copies):
        copy.start()


def recv(*copies):
    for copy in flat(copies):
        copy.wait_recv()


class Gather:
    def __init__(self, links, place, own, full, order, single=True, last=True):
        every = slice(None)
        y, other = place.y, place.other_y

        def same(device, k, yy, to):
            return links.add(device, full(k, every, yy), full(to, every, yy), Z_DEV)

        def along_z(k, yy, block):
            here, passed = full(k, place.z, yy), full(k, place.zs[2], yy)
            return [
                links.add(place.to_z[1], block, here),
                links.add(place.to_z[2], block, here),
                links.add(place.to_z[1], passed, passed),
            ]

        if order != WHOLE:
            self.z = along_z(0, y, own)
        if order == X_Z_Y:
            self.first = [links.add(place.to_x, own, full(2, place.z, y), 2)]
            self.far = along_z(2, y, full(2, place.z, y))
            blocks = [(0, y), (2, y), (0, other), (2, other)]
        else:
            blocks = [(0, y), (0, other), (2, y), (2, other)]
        if order == Y_Z_X:
            self.first = [links.add(place.to_y, own, full(0, place.z, y), 2)]
            self.far = along_z(0, other, full(0, place.z, other))
        if order == Z_Y_X and single:
            self.first = [same(place.to_y, 0, y, 0)]
        if order == Z_Y_X and not single:
            self.first = [links.add(place.to_y, own, full(0, place.z, y))]
            for k in range(1, 4):
                block = full(0, place.zs[k], y)
                self.first.append(links.add(place.to_y, block, block))
            return
        self.second = [
            same(place.to_y, k, yy, k) if order == X_Z_Y else same(place.to_x, k, yy, 2)
            for k, yy in blocks[: 2 if last else 1]
        ]
        if not last:
            blocks = [block for block in blocks if block[0] == 0]
        self.core = [same(place.to_core, k, yy, k + 1) for k, yy in blocks]


Z_Y_X, Y_Z_X, X_Z_Y, WHOLE = range(4)


def fused_forward(
    tie_ref, len_ref, tokens_ref, gains_ref, bias_ref, in_ref, out_ref, expand_ref,
    project_ref,
    gq_ref, gw_ref, flat1_ref, flat2_ref, rows_ref,
    q_ref, v_ref, kt_ref, p_ref, scale_ref, o_ref, a1t_out, h1_out, a2_out, a2t_out,
    own0_ref, ownw_ref, own1_ref, own2_ref, square_ref, vec_ref,
    all0_ref, allw_ref, w1_ref, w2_ref, vecs_ref, bqv_ref, x_ref, a1_ref, k_ref, qa_ref, vt_ref, ot_ref, a1t_ref, h1_ref, a2_ref, a2t_ref,
    send_sem, recv_sem, local_sem, flush_sem, row_sem,
):
    t, h = pl.program_id(0), pl.program_id(1)
    n, _ = x_ref.shape
    width = allw_ref.shape[-1]
    heads = width // HEAD_DIM
    step = 256
    place = Place()
    length = len_ref[place.t]
    links = Links(send_sem, recv_sem)
    z, y, x, c = place.z, place.y, place.x, place.c
    mine_there = vecs_ref.at[z, y, x, c]
    column = vecs_ref.at[:, :, x, c]
    vec_one = [links.add(device, vec_ref, mine_there) for device in place.same_t]
    vec_two = [links.add(device, column, column) for device in place.same_dp]
    half = own0_ref.shape[0] // 2
    halves = []
    for i in range(2):
        rows = pl.ds(i * half, half)
        halves.append(Gather(
            links, place, own0_ref.at[rows],
            lambda k, z, y, rows=rows: all0_ref.at[k, z, y, rows], Z_Y_X, single=False,
        ))
    seg0 = Gather(links, place, own0_ref, lambda k, z, y: all0_ref.at[k, z, y], WHOLE)
    segw = Gather(links, place, ownw_ref, lambda k, z, y: allw_ref.at[k, z, y], Z_Y_X)
    seg1 = Gather(
        links, place, own1_ref, lambda k, z, y: w1_ref.at[k, z, y], Y_Z_X, last=False
    )
    seg2 = Gather(
        links, place, own2_ref, lambda k, z, y: w2_ref.at[k, z, y], X_Z_Y, last=False
    )
    flush = [
        [
            pltpu.make_async_copy(ref.at[k], flat.at[k], flush_sem.at[i, k])
            for k in range(3)
        ]
        for i, (ref, flat) in enumerate([(w1_ref, flat1_ref), (w2_ref, flat2_ref)])
    ]
    put_a1t = pltpu.make_async_copy(a1t_ref, a1t_out, local_sem.at[0])
    put_a2t = pltpu.make_async_copy(a2t_ref, a2t_out, local_sem.at[1])
    puts = []
    for i in range(n // step):
        rows = pl.ds(i * step, step)
        puts.append([
            pltpu.make_async_copy(h1_ref.at[rows], h1_out.at[rows], row_sem.at[0, i]),
            pltpu.make_async_copy(a2_ref.at[rows], a2_out.at[rows], row_sem.at[1, i]),
        ])
    fetch = pltpu.make_async_copy(tokens_ref.at[place.t], x_ref, local_sem.at[2])

    def relay_z(copies):
        recv(copies[1])
        start(copies[2])

    def pass_own(seg):
        recv(seg.z[0], seg.z[2])
        if seg is segw:
            start(seg.first)
        start(seg.second[0], seg.core[0])

    def pass_second(seg):
        recv(seg.second)
        if seg is seg2:
            start(seg.core[1])

    def pass_first(seg):
        recv(seg.first)
        if seg is segw:
            start(seg.second[1], seg.core[1])
        else:
            start(seg.far[1], seg.far[0])

    def pass_far(seg):
        recv(seg.far[0], seg.far[2])
        start(seg.core[1:] if seg is seg1 else [])

    def pass_core(seg, i):
        recv(seg.second[i])
        start(seg.core[2 + i])

    plan = [
        (0, 0, lambda: (pass_own(segw), pass_first(seg1), relay_z(seg2.z), pass_first(seg2))),
        (0, 3, lambda: (pass_first(segw), relay_z(seg1.z), pass_core(seg0, 0))),
        (1, 0, lambda: recv(seg0.core[:2])),
        (1, 1, lambda: relay_z(seg1.far)),
        (1, 3, lambda: pass_core(seg0, 1)),
        (1, 4, lambda: (recv(segw.core[:2]), pass_core(segw, 0), pass_own(seg2))),
        (2, 1, lambda: relay_z(seg2.far)),
        (2, 2, lambda: pass_core(segw, 1)),
        (2, 3, lambda: pass_own(seg1)),
        (3, 0, lambda: (recv(seg0.core[2:]), pass_far(seg1), flush[0][0].start())),
        (3, 2, lambda: (pass_second(seg2), flush[1][0].start())),
        (3, 3, lambda: (pass_far(seg2), flush[1][2].start())),
        (3, 4, lambda: recv(segw.core[2:])),
    ]

    def serve(points):
        for step, where, act in plan:
            if where in points:
                now = (t == step) & (h == max(where - 2, 0))
                pl.when(now)(lambda act=act: (act(), None)[1])

    @pl.when((t == 0) & (h == 0))
    def _():
        s0, s1, s2, s3 = tie_ref[0], tie_ref[1], tie_ref[2], tie_ref[3]
        fetch.start()
        square_ref[...] = jnp.zeros_like(square_ref)
        gain = gains_ref.shape[-1]
        square_ref[0:1, :gain] = gains_ref[s0].astype(F32)[0:1]
        square_ref[1:2, :gain] = gains_ref[s2].astype(F32)[1:2]
        kinds = [s0, s0, s0, s1, s2, s3, s2, s2, s2, s2]
        for i, source in enumerate(kinds):
            wide = bias_ref[i].astype(F32)
            here = lax.broadcasted_iota(jnp.int32, wide.shape, 0) == source
            square_ref[2 + i : 3 + i, :gain] = jnp.sum(
                jnp.where(here, wide, 0.0), 0, keepdims=True
            )
        vec_ref[...] = square_ref[...].T[:gain]
        for j in range(3):
            own0_ref[:, j * width : (j + 1) * width] = in_ref[s0, j]
        place.greet(place.same_t + place.same_dp)
        start(vec_one)
        for part in halves:
            start(part.z[1], part.z[0], part.first[0])
        vecs_ref[z, y, x, c] = vec_ref[...]
        ones = lax.broadcasted_iota(jnp.int32, (vt_ref.shape[1] - HEAD_DIM, n), 0) == 0
        for h in range(heads):
            vt_ref[h, HEAD_DIM:, :] = ones.astype(BF16)
        all0_ref[0, z, y] = own0_ref[...]
        ownw_ref[...] = out_ref[s1].T
        allw_ref[0, z, y] = ownw_ref[...]
        own1_ref[...] = expand_ref[s2]
        own2_ref[...] = project_ref[s3]
        w1_ref[0, z, y] = own1_ref[...]
        w2_ref[0, z, y] = own2_ref[...]
        recv(vec_one)
        start(vec_two)
        for part in halves:
            relay_z(part.z)
            start(part.first[2])
        for part in halves:
            recv(part.z[0])
            start(part.first[1])
        start(segw.z[1], segw.z[0], seg2.z[1])
        recv(vec_two)
        start(seg2.first)
        vecs = vecs_ref[...].reshape(D, vecs_ref.shape[-1]).T[:16]
        rows_ref[...] = vecs
        for part in halves:
            recv(part.z[2])
            start(part.first[3])
        start(seg1.first, seg0.second[0], seg0.core[0])
        for k in range(4):
            part = slice(k * width, (k + 1) * width)
            bqv_ref[k, 0:1, :width] = vecs[3:4, part]
            bqv_ref[k, 0:1, width : 2 * width] = jnp.zeros((1, width), F32)
            bqv_ref[k, 0:1, 2 * width :] = vecs[4:5, part]
        fetch.wait()

        @pl.loop(0, n // step)
        def _(b):
            rows = pl.ds(pl.multiple_of(b * step, step), step)
            wide = x_ref[rows, :].astype(F32)
            xhat, _ = norm_parts(wide)
            a1 = (xhat * rows_ref[0:1, :] + rows_ref[2:3, :]).astype(BF16)
            a1_ref[rows, :] = a1
            a1t_ref[:, rows] = a1.T
            h1_ref[rows, :] = wide + rows_ref[5:6, :]

        put_a1t.start()
        relay_z(segw.z)
        start(seg2.z[0], seg1.z[1], seg1.z[0])
        recv(halves[0].first, halves[1].first)
        start(seg0.second[1], seg0.core[1])

    serve([0])

    @pl.when(h == 0)
    def _():
        gq = all0_ref[t].reshape(D, 3 * width)
        gq_ref[0] = gq
        mine = place.group(t)
        qkv = dot_nn(a1_ref[...], gq) + bqv_ref[mine, 0:1, :]
        q = qkv[:, :width].astype(BF16) * jnp.asarray(HEAD_DIM ** -0.5, BF16)
        k = qkv[:, width : 2 * width].astype(BF16)
        v = qkv[:, 2 * width :].astype(BF16)
        q_ref[0] = q
        kt_ref[0] = k.T
        v_ref[0] = v
        vt = v.T
        for h in range(heads):
            vt_ref[h, :HEAD_DIM, :] = vt[h * HEAD_DIM : (h + 1) * HEAD_DIM]
        spare = k_ref.shape[1] - width
        dead = lax.broadcasted_iota(jnp.int32, (n, spare), 0) >= length
        first_column = lax.broadcasted_iota(jnp.int32, (n, spare), 1) == 0
        k_ref[:, :width] = k
        k_ref[:, width:] = jnp.where(first_column & dead, MASKED, 0.0).astype(BF16)
        qa_ref[:, :width] = q
        qa_ref[:, width:] = jnp.where(first_column, 1.0, 0.0).astype(BF16)
        scale_ref[0, heads:, :] = jnp.zeros((scale_ref.shape[1] - heads, n), F32)

    serve([1])

    lane = lax.broadcasted_iota(jnp.int32, (1, qa_ref.shape[1]), 1)
    keep = ((lane >= h * HEAD_DIM) & (lane < (h + 1) * HEAD_DIM)) | (lane >= width)
    key = lax.broadcasted_iota(jnp.int32, (step, step), 0)
    query = lax.broadcasted_iota(jnp.int32, (step, step), 1)
    head = pl.ds(pl.multiple_of(h * HEAD_DIM, HEAD_DIM), HEAD_DIM)

    def scores(b):
        first, last = b * step, (b + 1) * step
        q = jnp.where(keep, qa_ref[first:last, :], jnp.zeros((), BF16))
        return dot_nt(k_ref[:last, :], q)

    def attend(b, s):
        first, last = b * step, (b + 1) * step
        near = jnp.where(key <= query, s[first:], MASKED)
        top = jnp.max(near, 0, keepdims=True)
        if b:
            far = s[:first]
            top = jnp.maximum(top, jnp.max(far, 0, keepdims=True))
        e_near = jnp.exp((near - top).astype(BF16))
        p_ref[0, 0, b, first:last, :] = e_near
        o = dot_nn(vt_ref[h, :, first:last], e_near)
        if b:
            e_far = jnp.exp((far - top).astype(BF16))
            p_ref[0, 0, b, :first, :] = e_far
            o += dot_nn(vt_ref[h, :, :first], e_far)
        scale = 1.0 / o[HEAD_DIM : HEAD_DIM + 1]
        scale_ref[0, pl.ds(h, 1), first:last] = scale
        ot_ref[head, first:last] = (o[:HEAD_DIM] * scale).astype(BF16)

    s = scores(0)
    for b in range(n // step):
        ahead = scores(b + 1) if b + 1 < n // step else None
        attend(b, s)
        s = ahead

    serve([2, 3, 4])

    @pl.when(h == heads - 1)
    def _():
        gw_ref[0] = allw_ref[t].reshape(gw_ref.shape[1:])
        o = ot_ref[...].T
        o_ref[0] = o
        h1_ref[...] += dot_nt(o, gw_ref[0])

    @pl.when((t == 3) & (h == heads - 1))
    def _():
        for i, rows in enumerate(blocks(n, step)):
            xhat, _ = norm_parts(h1_ref[rows, :])
            a2 = (xhat * rows_ref[1:2, :] + rows_ref[6:7, :]).astype(BF16)
            a2_ref[rows, :] = a2
            a2t_ref[:, rows] = a2.T
            for put in puts[i]:
                put.start()
        put_a2t.start()
        recv(seg2.core)
        flush[1][1].start()
        recv(seg1.core)
        flush[0][1].start()
        pass_second(seg1)
        flush[0][2].start()
        links.sent()
        for copies in flush + puts + [[put_a1t, put_a2t]]:
            for copy in copies:
                copy.wait()


N_GATHER = 10 + 14 + 6 + 10 + 10 + 10
VMEM_WHOLE = pl.BlockSpec(memory_space=pltpu.VMEM)
ANY_WHOLE = pl.BlockSpec(memory_space=pl.ANY)


def run_fused_forward(tie, lengths, tokens, gains, biases, w_in, w_out, w_expand, w_project):
    groups, n, _ = tokens.shape
    depth, width = w_in.shape[-2:]
    heads = width // HEAD_DIM
    hidden = w_expand.shape[-1]
    w_project = w_project.transpose(0, 2, 1)
    biases = biases.transpose(1, 0, 2)
    own = gains.shape[-1]

    def group(*shape):
        return pl.BlockSpec((1,) + shape, lambda t, h: (t,) + (0,) * len(shape))

    per_head = pl.BlockSpec((1, 1, n // 256, n, 256), lambda t, h: (t, h, 0, 0, 0))
    return pl.pallas_call(
        fused_forward,
        grid=(groups, heads),
        in_specs=[SMEM_WHOLE, SMEM_WHOLE, ANY_WHOLE] + [VMEM_WHOLE] * 6,
        out_specs=[
            group(D, 3 * width), group(D, width), ANY_WHOLE, ANY_WHOLE, VMEM_WHOLE,
            group(n, width), group(n, width), group(width, n), per_head,
            group(8, n), group(n, width), ANY_WHOLE, ANY_WHOLE, ANY_WHOLE, ANY_WHOLE,
        ],
        out_shape=[
            shaped(BF16, groups, D, 3 * width), shaped(BF16, groups, D, width),
            shaped(BF16, groups, Z_DEV, Y_DEV, depth, hidden),
            shaped(BF16, groups, Z_DEV, Y_DEV, depth, hidden),
            shaped(F32, 16, D),
            shaped(BF16, groups, n, width), shaped(BF16, groups, n, width),
            shaped(BF16, groups, width, n), shaped(BF16, groups, heads, n // 256, n, 256),
            shaped(F32, groups, 8, n), shaped(BF16, groups, n, width), shaped(BF16, D, n), shaped(F32, n, D),
            shaped(BF16, n, D), shaped(BF16, D, n),
        ],
        scratch_shapes=[
            pltpu.VMEM((depth, 3 * width), BF16), pltpu.VMEM((depth, width), BF16),
            pltpu.VMEM((depth, hidden), BF16), pltpu.VMEM((depth, hidden), BF16),
            pltpu.VMEM((128, 128), F32), pltpu.VMEM((own, 128), F32),
            pltpu.VMEM((groups, Z_DEV, Y_DEV, depth, 3 * width), BF16),
            pltpu.VMEM((groups, Z_DEV, Y_DEV, depth, width), BF16),
            pltpu.VMEM((groups, Z_DEV, Y_DEV, depth, hidden), BF16),
            pltpu.VMEM((groups, Z_DEV, Y_DEV, depth, hidden), BF16),
            pltpu.VMEM((Z_DEV, Y_DEV, X_DEV, C_DEV, own, 128), F32),
            pltpu.VMEM((groups, 8, 3 * width), F32),
            pltpu.VMEM((n, D), BF16), pltpu.VMEM((n, D), BF16), pltpu.VMEM((n, 256), BF16),
            pltpu.VMEM((n, 256), BF16), pltpu.VMEM((heads, HEAD_DIM + 16, n), BF16),
            pltpu.VMEM((width, n), BF16),
            pltpu.VMEM((D, n), BF16), pltpu.VMEM((n, D), F32), pltpu.VMEM((n, D), BF16),
            pltpu.VMEM((D, n), BF16),
            pltpu.SemaphoreType.DMA((N_GATHER,)), pltpu.SemaphoreType.DMA((N_GATHER,)),
            pltpu.SemaphoreType.DMA((3,)), pltpu.SemaphoreType.DMA((2, 4)),
            pltpu.SemaphoreType.DMA((2, n // 256)),
        ],
        compiler_params=pltpu.CompilerParams(
            vmem_limit_bytes=VMEM_LIMIT, collective_id=0, has_side_effects=True
        ),
        name="fused_forward",
    )(tie, lengths, tokens, gains, biases, w_in, w_out, w_expand, w_project)


class Result:
    def __init__(self, links, place, own_ref, passing_ref, out_ref, step, sem, count):
        self.x, self.core, self.far, self.keep, self.keep_far = [], [], [], [], []
        for i in range(count):
            rows = pl.ds(i * step, step)
            mine, theirs = out_ref.at[place.t, rows], out_ref.at[place.ts[2], rows]
            own, passing = own_ref.at[rows], passing_ref.at[rows]
            self.x.append(links.add(place.to_x, own, passing))
            self.core.append(links.add(place.to_core, own, mine))
            self.far.append(links.add(place.to_core, passing, theirs))
            self.keep.append(pltpu.make_async_copy(own, mine, sem.at[0, i]))
            self.keep_far.append(pltpu.make_async_copy(passing, theirs, sem.at[1, i]))

    def send(self, i):
        start(self.x[i], self.core[i], self.keep[i])

    def pass_on(self, i):
        recv(self.x[i])
        start(self.far[i], self.keep_far[i])

    def finish(self):
        recv(self.core, self.far)
        for copy in self.keep + self.keep_far:
            copy.wait()


def low(value):
    return jnp.asarray(value, BF16)


def pair_order(i):
    return i + 1 - 2 * (i % 2)


def fused_feed_forward(
    len_ref, cot_ref, a2_ref, a2t_in, h1_in, far1_ref, far2_ref, rows_ref,
    out_out, fold_ref, work_out, dh1_out, gb_out, gbt_out, sums_ref,
    gf_ref, gft_ref, feed_ref, da2_ref, h_ref, df_ref, weights_ref, missing_ref, third_ref,
    stage_ref, land_ref, near_ref, cross_ref, a2t_ref, h1_ref, out_ref, work_ref,
    send_sem, recv_sem, local_sem, row_sem,
):
    t = pl.program_id(0)
    n = gf_ref.shape[0]
    step = 256
    depth = stage_ref.shape[-2]
    place = Place()
    length = len_ref[place.t]
    links = Links(send_sem, recv_sem)
    y, other = place.y, place.other_y
    last = [
        links.add(place.to_x, far1_ref.at[0, :, other], missing_ref.at[0, 0]),
        links.add(place.to_y, far2_ref.at[2, :, y], missing_ref.at[1, 0]),
    ]
    last_core = [
        links.add(place.to_core, missing_ref.at[i, 0], missing_ref.at[i, 1]) for i in range(2)
    ]
    third = [
        links.add(place.to_core, far_ref.at[2, :, y], third_ref.at[i])
        for i, far_ref in enumerate([far1_ref, far2_ref])
    ]
    core = [
        [links.add(place.to_core, stage_ref.at[i], land_ref.at[s, i]) for i in range(2)]
        for s in range(2)
    ]
    cross = [
        links.add(place.to_y, near_ref.at[i, :, other], cross_ref.at[i]) for i in range(2)
    ]
    fetch = pltpu.make_async_copy(cot_ref.at[place.t], gf_ref, local_sem.at[0])
    gb_ref, gbt_ref, dh1_ref = gf_ref, gft_ref, da2_ref
    late = [
        pltpu.make_async_copy(a2t_in, a2t_ref, local_sem.at[5]),
        pltpu.make_async_copy(h1_in, h1_ref, local_sem.at[6]),
    ]
    puts = []
    for i in range(n // step):
        rows = pl.ds(i * step, step)
        puts.append([
            pltpu.make_async_copy(ref.at[rows], out.at[rows], row_sem.at[j, i])
            for j, (ref, out) in enumerate(
                [(out_ref, out_out), (dh1_ref, dh1_out), (gb_ref, gb_out)]
            )
        ])
    put_gbt = pltpu.make_async_copy(gbt_ref, gbt_out, local_sem.at[7])
    put_work = pltpu.make_async_copy(work_ref, work_out, local_sem.at[8])
    k = pair_order(t)
    mine = place.group(k)

    def load(step, whole, slot):
        for i, far_ref in enumerate([far1_ref, far2_ref]):
            group = far_ref.at[pair_order(step)]
            to = weights_ref.at[slot, i]
            if not whole:
                group, to = group.at[:, y], to.at[:, y]
            yield pltpu.make_async_copy(group, to, local_sem.at[1 + 2 * slot + i])

    def live_rows(b):
        at = b * step + lax.broadcasted_iota(jnp.int32, (step, 1), 0)
        return (at < length).astype(F32)

    @pl.when(t == 0)
    def _():
        fetch.start()
        for copy in load(0, True, 0):
            copy.start()
        for copy in late:
            copy.start()
        place.greet()
        start(last, third)
        sums_ref[...] = jnp.zeros_like(sums_ref)
        feed_ref[...] = jnp.zeros_like(feed_ref)
        da2_ref[...] = jnp.zeros_like(da2_ref)
        fetch.wait()

        @pl.loop(0, n // step)
        def _(b):
            rows = pl.ds(pl.multiple_of(b * step, step), step)
            g = (gf_ref[rows, :].astype(F32) * live_rows(b)).astype(BF16)
            gf_ref[rows, :] = g
            gft_ref[:, rows] = g.T
            sums_ref[7:8, :] += jnp.sum(g.astype(F32), 0, keepdims=True)

    for i in range(4):
        @pl.when(t == i)
        def _():
            if i == 2:
                recv(last_core, third)
            else:
                for copy in load(i, i < 2, i % 2):
                    copy.wait()
            if i in (0, 2):
                for copy in load(i + 1, i + 1 < 2, (i + 1) % 2):
                    copy.start()
            for j in range(2):
                if i == 2:
                    weights_ref[0, j, :, y] = third_ref[j]
                if i >= 2:
                    weights_ref[i % 2, j, :, other] = missing_ref[j, 3 - i]

    bias = rows_ref[pl.ds(8 + mine, 1), :]
    w1 = weights_ref[t % 2, 0].reshape(D, -1)
    w2 = weights_ref[t % 2, 1].reshape(D, -1)
    column = jnp.zeros((1, w1.shape[1]), F32)
    for rows in blocks(n, step):
        f = (dot_nn(a2_ref[rows, :], w1) + bias).astype(BF16)
        dh = dot_nn(gf_ref[rows, :], w2)
        f2 = f * f
        th = jnp.tanh(f * (low(SQRT_2_PI) + low(SQRT_2_PI * 0.044715) * f2))
        half = low(0.5) + low(0.5) * th
        h = f * half
        slope = half + f * (low(0.5) - low(0.5) * th * th) * (
            low(SQRT_2_PI) + low(3 * SQRT_2_PI * 0.044715) * f2
        )
        df = (dh * slope.astype(F32)).astype(BF16)
        h_ref[rows, :] = h
        df_ref[rows, :] = df
        column += jnp.sum(df.astype(F32), 0, keepdims=True)
        feed_ref[rows, :] += dot_nt(h, w2)
        da2_ref[rows, :] += dot_nt(df, w1)
    sums_ref[pl.ds(8 + mine, 1), :] = column

    @pl.when(t == 1)
    def _():
        recv(last)
        start(last_core)

    @pl.when(t == 0)
    def _():
        late[0].wait()

    def weight_grad(left_ref, right_ref):
        value = dot_nn(left_ref[...], right_ref[...])
        return value.reshape(Z_DEV, Y_DEV, depth, value.shape[-1]).astype(BF16)

    grad1 = weight_grad(a2t_ref, df_ref)
    grad2 = weight_grad(gft_ref, h_ref)

    def put(ref):
        ref[0] = grad1
        ref[1] = grad2

    def reduced(ref):
        return lambda i, s, z: (
            ref[i, z].astype(F32) + land_ref[s, i, z].astype(F32)
        ).astype(BF16)

    @pl.when(t == 0)
    def _():
        put(stage_ref)
        start(core[0])

    @pl.when(t == 1)
    def _():
        put(near_ref)
        recv(core[0])

        @pl.loop(0, Z_DEV)
        def _(z):
            for i in range(2):
                near_ref[i, z] = reduced(near_ref)(i, 0, z)

        start(cross)

    @pl.when(t == 2)
    def _():
        for copy in core[0]:
            copy.wait_send()
        put(stage_ref)
        start(core[1])

    @pl.when(t == 3)
    def _():
        put(work_ref)
        late[1].wait()
        for i, rows in enumerate(blocks(n, step)):
            live = live_rows(i)
            h1 = h1_ref[rows, :]
            out_ref[rows, :] = (live * (h1 + (feed_ref[rows, :] + rows_ref[7:8, :]))).astype(BF16)
            xhat, r = norm_parts(h1)
            da2 = da2_ref[rows, :]
            sums_ref[1:2, :] += jnp.sum(da2 * xhat, 0, keepdims=True)
            sums_ref[6:7, :] += jnp.sum(da2, 0, keepdims=True)
            dg = da2 * rows_ref[1:2, :]
            dv = r * (
                dg
                - jnp.mean(dg, -1, keepdims=True)
                - xhat * jnp.mean(dg * xhat, -1, keepdims=True)
            )
            dh1 = gf_ref[rows, :].astype(F32) + dv
            dh1_ref[rows, :] = dh1
            gb = dh1.astype(BF16)
            gb_ref[rows, :] = gb
            gbt_ref[:, rows] = gb.T
            sums_ref[5:6, :] += jnp.sum(gb.astype(F32), 0, keepdims=True)
            for copy in puts[i]:
                copy.start()
        put_gbt.start()
        recv(core[1])

        @pl.loop(0, Z_DEV)
        def _(z):
            for i in range(2):
                work_ref[i, z] = reduced(work_ref)(i, 1, z)

        put_work.start()
        recv(cross)

        @pl.loop(0, Z_DEV)
        def _(z):
            for i in range(2):
                fold_ref[i, z] = (
                    near_ref[i, z, y].astype(F32) + cross_ref[i, z].astype(F32)
                ).astype(BF16)

        links.sent(*core[0])
        for copies in puts + [[put_gbt, put_work]]:
            for copy in copies:
                copy.wait()


def run_fused_feed_forward(lengths, cot, a2, a2t, h1, g1, g2, rows):
    n = cot.shape[1]
    groups, _, _, depth, hidden = g1.shape
    both = (2, Z_DEV, Y_DEV, depth, hidden)
    fold = (2, Z_DEV, depth, hidden)
    return pl.pallas_call(
        fused_feed_forward,
        grid=(groups,),
        in_specs=[SMEM_WHOLE, ANY_WHOLE, VMEM_WHOLE] + [ANY_WHOLE] * 4 + [VMEM_WHOLE],
        out_specs=[ANY_WHOLE, VMEM_WHOLE] + [ANY_WHOLE] * 4 + [VMEM_WHOLE],
        out_shape=[
            shaped(BF16, n, D), shaped(BF16, *fold), shaped(BF16, *both), shaped(F32, n, D),
            shaped(BF16, n, D), shaped(BF16, D, n), shaped(F32, 16, D),
        ],
        scratch_shapes=[
            pltpu.VMEM((n, D), BF16), pltpu.VMEM((D, n), BF16), pltpu.VMEM((n, D), F32),
            pltpu.VMEM((n, D), F32), pltpu.VMEM((n, hidden), BF16), pltpu.VMEM((n, hidden), BF16),
            pltpu.VMEM((2,) + both, BF16),
            pltpu.VMEM((2,) + fold, BF16), pltpu.VMEM(fold, BF16), pltpu.VMEM(both, BF16),
            pltpu.VMEM((2,) + both, BF16),
            pltpu.VMEM(both, BF16), pltpu.VMEM(fold, BF16),
            pltpu.VMEM((D, n), BF16), pltpu.VMEM((n, D), F32), pltpu.VMEM((n, D), BF16),
            pltpu.VMEM(both, BF16),
            pltpu.SemaphoreType.DMA((12,)), pltpu.SemaphoreType.DMA((12,)),
            pltpu.SemaphoreType.DMA((9,)), pltpu.SemaphoreType.DMA((3, n // 256)),
        ],
        compiler_params=pltpu.CompilerParams(
            vmem_limit_bytes=VMEM_LIMIT, collective_id=1, has_side_effects=True
        ),
        name="fused_feed_forward",
    )(lengths, cot, a2, a2t, h1, g1, g2, rows)
class Reduce:
    def __init__(
        self, links, place, work, acc, cross_ref, far_ref, mid_ref, last_ref, side_ref,
        slots=(0, 1), split=False,
    ):
        self.place, self.work, self.acc = place, work, acc
        self.cross_ref, self.far_ref, self.mid_ref = cross_ref, far_ref, mid_ref
        self.last_ref, self.side_ref = last_ref, side_ref
        self.two = len(slots) == 2
        zs = place.zs
        self.y = {
            s: [
                links.add(
                    place.to_y, work(s, zs[j], place.other_y),
                    cross_ref.at[s if self.two else 0, zs[j]],
                )
                for j in (1, 3, 2, 0)
            ]
            for s in slots
        }
        self.z = [
            [
                links.add(place.to_z[1], acc(s, zs[1]), far_ref.at[s, 0]),
                links.add(place.to_z[1], acc(s, zs[3]), far_ref.at[s, 1]),
                links.add(place.to_z[2], mid_ref.at[s, 1], far_ref.at[s, 2]),
            ]
            for s in range(1 if split else 2)
        ]
        self.x = links.add(place.to_x, last_ref, side_ref)

    def fold_y(self, s, half):
        for i, j in [(0, 1), (1, 3), (2, 2), (3, 0)][2 * half : 2 * half + 2]:
            z = self.place.zs[j]
            recv(self.y[s][i])
            value = self.work(s, z, self.place.y)[...].astype(F32)
            cross = self.cross_ref[s if self.two else 0, z].astype(F32)
            self.acc(s, z)[...] = (value + cross).astype(BF16)
            if i < 2:
                start(self.z[s][i])

    def fold_z(self, s):
        recv(self.z[s][:2])
        for i in (1, 0):
            value = self.acc(s, self.place.zs[2 * i])[...].astype(F32)
            self.mid_ref[s, i] = (value + self.far_ref[s, i].astype(F32)).astype(BF16)
            if i:
                start(self.z[s][2])

    def own(self, s):
        recv(self.z[s][2])
        return self.mid_ref[s, 0].astype(F32) + self.far_ref[s, 2].astype(F32)

    def send_x(self):
        self.last_ref[...] = self.own(1).astype(BF16)
        start(self.x)

    def total(self):
        value = self.own(0)
        recv(self.x)
        return value + self.side_ref[...].astype(F32)


class ReduceHalves:
    def __init__(self, links, place, work, landings, last_ref):
        self.place, self.work = place, work
        self.cross, self.far, self.mid, self.far2, self.mid2, self.fin2, self.cross2 = landings
        self.last_ref = last_ref
        zs, half = place.zs, last_ref.shape[0] // 2
        self.low, self.high = pl.ds(0, half), pl.ds(half, half)
        every = slice(None)
        y, other = place.y, place.other_y
        self.y = [
            links.add(place.to_y, work.at[zs[j], other, self.low], self.cross.at[zs[j]])
            for j in (1, 3, 2, 0)
        ]
        self.z = [
            links.add(place.to_z[1], work.at[zs[1], y, self.low], self.far.at[0]),
            links.add(place.to_z[1], work.at[zs[3], y, self.low], self.far.at[1]),
            links.add(place.to_z[2], self.mid.at[1], self.far.at[2]),
        ]
        self.z2 = [
            links.add(place.to_z[1], work.at[zs[1], every, self.high], self.far2.at[0]),
            links.add(place.to_z[1], work.at[zs[3], every, self.high], self.far2.at[1]),
            links.add(place.to_z[2], self.mid2.at[1], self.far2.at[2]),
        ]
        self.y2 = links.add(place.to_y, self.fin2.at[other], self.cross2)

    def begin(self):
        start(self.y, self.z2[:2])

    def add(self, target, left, right):
        target[...] = (left[...].astype(F32) + right[...].astype(F32)).astype(BF16)

    def fold_y(self):
        y, zs = self.place.y, self.place.zs
        for i, j in enumerate((1, 3, 2, 0)):
            recv(self.y[i])
            block = self.work.at[zs[j], y, self.low]
            self.add(block, block, self.cross.at[zs[j]])
            if i < 2:
                start(self.z[i])

    def fold_high(self):
        recv(self.z2[:2])
        for i in (1, 0):
            block = self.work.at[self.place.zs[2 * i], :, self.high]
            self.add(self.mid2.at[i], block, self.far2.at[i])
            if i:
                start(self.z2[2])

    def cross_high(self):
        recv(self.z2[2])
        self.add(self.fin2, self.mid2.at[0], self.far2.at[2])
        start(self.y2)

    def fold_z(self):
        recv(self.z[:2])
        for i in (1, 0):
            block = self.work.at[self.place.zs[2 * i], self.place.y, self.low]
            self.add(self.mid.at[i], block, self.far.at[i])
            if i:
                start(self.z[2])

    def finish(self):
        recv(self.z[2])
        self.add(self.last_ref.at[self.low], self.mid.at[0], self.far.at[2])
        recv(self.y2)
        self.add(self.last_ref.at[self.high], self.fin2.at[self.place.y], self.cross2)


def fused_backward(
    tokens_ref, gq_in, gw_in, rows_ref, dh1_ref, gb_ref, gbt_in, q_in, v_in, kt_in,
    p_ref, scale_in, o_in, a1t_in, layer_in, fold_in, work_in, early_ref,
    out_ref, layerout_ref, part0_ref, partw_ref, part1_ref, part2_ref, total_ref,
    gq_ref, gw_ref, q_ref, v_ref, kt_ref, scale_ref, o_ref,
    a1t_ref, gbt_ref, layer_ref, fold_ref, work_ref, do_ref, delta_ref, dkv_ref, dqkv_ref, da1_ref, own_ref, passing_ref, passlayer_ref, bqv_ref,
    folded_ref, cross1_ref, far1_ref, mid1_ref, last1_ref, side1_ref,
    cross2_ref, far2_ref, mid2_ref, last2_ref, side2_ref,
    stagew_ref, landw_ref, workw_ref, crossw_ref, farw_ref, midw_ref, lastw_ref, sidew_ref,
    stage0_ref, land0_ref, work0_ref, cross0_ref, far0_ref, mid0_ref, last0_ref, side0_ref,
    sums_ref, sumland_ref,
    send_sem, recv_sem, local_sem, result_sem, group_sem, *tail_refs,
):
    t = pl.program_id(0)
    n = own_ref.shape[0]
    width = gw_ref.shape[-1]
    depth = part0_ref.shape[0]
    heads = width // HEAD_DIM
    step = n // 4
    place = Place()
    y = place.y
    links = Links(send_sem, recv_sem)
    k, i = group_and_block(t)
    mine = place.group(k)
    now = k % 2
    out = Result(links, place, own_ref, passing_ref, out_ref, step, result_sem.at[0], 4)
    layer = Result(links, place, layer_ref, passlayer_ref, layerout_ref, step, result_sem.at[1], 4)
    fetch = pltpu.make_async_copy(tokens_ref.at[place.t], own_ref, local_sem.at[0])
    fetch_layer, fetch_work, fetch_fold, fetch_gbt, fetch_a1t = [
        pltpu.make_async_copy(there, here, local_sem.at[1 + j])
        for j, (there, here) in enumerate([
            (layer_in, layer_ref), (work_in, work_ref), (fold_in, fold_ref),
            (gbt_in, gbt_ref), (a1t_in, a1t_ref),
        ])
    ]
    def operands(group):
        slot = group % 2
        pairs = [
            (gw_in, gw_ref), (scale_in, scale_ref), (o_in, o_ref), (v_in, v_ref),
            (q_in, q_ref), (kt_in, kt_ref), (gq_in, gq_ref),
        ]
        return [
            pltpu.make_async_copy(there.at[group], here.at[slot], group_sem.at[slot, j])
            for j, (there, here) in enumerate(pairs)
        ]

    corew = [links.add(place.to_core, stagew_ref, landw_ref.at[i]) for i in range(2)]
    core0 = [links.add(place.to_core, stage0_ref, land0_ref.at[i]) for i in range(2)]
    def half_done(i, *landing):
        return Reduce(
            links, place, lambda s, z, y: work_ref.at[i, z, y],
            lambda s, z: folded_ref.at[i, z] if s else fold_ref.at[i, z],
            *landing, slots=(1,),
        )

    seg1 = half_done(0, cross1_ref, far1_ref, mid1_ref, last1_ref, side1_ref)
    seg2 = half_done(1, cross2_ref, far2_ref, mid2_ref, last2_ref, side2_ref)
    segw = Reduce(
        links, place, lambda s, z, y: workw_ref.at[s, z, y],
        lambda s, z: workw_ref.at[s, z, y],
        crossw_ref, farw_ref, midw_ref, lastw_ref, sidew_ref,
    )
    seg0 = Reduce(
        links, place, lambda s, z, y: work0_ref.at[s, z, y],
        lambda s, z: work0_ref.at[s, z, y],
        cross0_ref, far0_ref, mid0_ref, last0_ref, side0_ref, slots=(0,), split=True,
    )
    tail = ReduceHalves(links, place, work0_ref.at[1], tail_refs, last0_ref)
    sum_core, sum_y, *sum_z, sum_x = [
        links.add(to, sums_ref.at[i], sumland_ref.at[j])
        for j, (i, to) in enumerate(
            zip([0, 1, 2, 2, 2, 3], [place.to_core, place.to_y] + place.to_z[1:] + [place.to_x])
        )
    ]

    early_copies = [
        corew[1], core0[1], *segw.y[0], *segw.y[1], *segw.z[0], *seg0.y[0], *seg0.z[0],
        out.x[3], out.core[3], *layer.x, *layer.core, *layer.far, seg1.x, seg2.x,
    ]
    for seg in (seg1, seg2):
        early_copies += [*seg.y[1], *seg.z[0], *seg.z[1]]

    def sent(copies):
        for copy in copies:
            copy.wait_send()

    def when(point):
        return pl.when(t == point)

    @when(0)
    def _():
        start(fetch_layer, operands(1), fetch_work, fetch_fold, fetch_gbt, operands(0))
        start(fetch, fetch_a1t)
        place.greet()
        fetch_layer.wait()
        for i in range(4):
            layer.send(i)
        fetch_work.wait()
        start(seg1.y[1], seg2.y[1])
        fetch_fold.wait()
        start(seg1.z[0][:2], seg2.z[0][:2])
        bqv_ref[...] = jnp.zeros_like(bqv_ref)
        sums_ref[0] = early_ref[...]
        fetch_gbt.wait()

    def add_core():
        recv(corew[1])

        @pl.loop(0, Z_DEV)
        def _(z):
            workw_ref[1, z] = (
                workw_ref[1, z].astype(F32) + landw_ref[1, z].astype(F32)
            ).astype(BF16)

        start(segw.y[1])

    def wait(copies):
        for copy in copies:
            copy.wait()

    @when(0)
    def _():
        wait(operands(1))

    @when(4)
    def _():
        start(operands(3))
        wait(operands(0))

    @when(8)
    def _():
        start(operands(2))
        wait(operands(3))

    @when(9)
    def _():
        wait(operands(2))

    plan = [
        (2, 1, lambda: (seg1.fold_y(1, 0), seg1.fold_z(0))),
        (3, 1, lambda: layer.pass_on(0)),
        (4, 0, lambda: (seg1.fold_y(1, 1), seg2.fold_z(0))),
        (4, 1, lambda: layer.pass_on(1)),
        (5, 1, lambda: (seg1.fold_z(1), seg2.fold_y(1, 0))),
        (8, 0, lambda: (seg2.fold_y(1, 1), layer.pass_on(2))),
        (8, 1, lambda: (seg1.send_x(), segw.fold_y(0, 0), segw.fold_y(0, 1))),
        (9, 0, add_core),
        (9, 1, lambda: (seg2.fold_z(1), seg0.fold_y(0, 0), layer.pass_on(3))),
        (10, 1, lambda: segw.fold_z(0)),
        (11, 1, lambda: (seg2.send_x(), seg0.fold_y(0, 1))),
        (12, 1, lambda: (segw.fold_y(1, 0), segw.fold_y(1, 1))),
        (13, 1, lambda: (seg0.fold_z(0), out.pass_on(3))),
        (14, 1, lambda: segw.fold_z(1)),
    ]

    def serve(point):
        for at, where, act in plan:
            if where == point:
                pl.when(t == at)(lambda act=act: (act(), None)[1])

    @pl.when((t == 0) | (t == 4) | (t == 8) | (t == 9))
    def _():
        pick = (
            lax.broadcasted_iota(jnp.int32, (8, width), 1) // HEAD_DIM
            == lax.broadcasted_iota(jnp.int32, (8, width), 0)
        ).astype(BF16)

        @pl.loop(0, n // step)
        def _(i):
            rows = pl.ds(pl.multiple_of(i * step, step), step)
            columns = scale_ref[now, :, rows].T
            lane = lax.broadcasted_iota(jnp.int32, (step, width), 1)
            scale = columns[:, heads - 1 : heads]
            for h in reversed(range(heads - 1)):
                scale = jnp.where(lane < (h + 1) * HEAD_DIM, columns[:, h : h + 1], scale)
            do = (dot_nn(gb_ref[rows, :], gw_ref[now]) * scale).astype(BF16)
            do_ref[now, rows, :] = do
            product = do.astype(F32) * o_ref[now, rows, :].astype(F32)
            high = product.astype(BF16)
            low = (product - high.astype(F32)).astype(BF16)
            delta_ref[now, :, rows] = dot_nt(pick, high) + dot_nt(pick, low)

        value = dot_nn(gbt_ref[...], o_ref[now]).reshape(Z_DEV, Y_DEV, depth, width)
        for s in range(2):
            @when(8 * s)
            def _():
                if s:
                    corew[0].wait_send()
                stagew_ref[...] = value.astype(BF16)
                start(corew[s])

        @when(4)
        def _():
            recv(corew[0])
            workw_ref[0] = (value + landw_ref[0].astype(F32)).astype(BF16)
            start(segw.y[0])

        @when(9)
        def _():
            workw_ref[1] = value.astype(BF16)

    serve(0)

    for ii in reversed(range(4)):
        @pl.when(i == ii)
        def _():
            first, last = ii * step, (ii + 1) * step
            do = do_ref[now, first:last, :]
            q = q_ref[now, first:last, :]
            v = v_ref[now, :last, :]
            lane = lax.broadcasted_iota(jnp.int32, (1, width), 1)
            dk, dv, dq = None, None, []
            for h in range(heads):
                low, high = h * HEAD_DIM, (h + 1) * HEAD_DIM
                here = (lane >= low) & (lane < high)
                p = p_ref[0, h, 0, :last, :]
                dp = dot_nt(v, jnp.where(here, do, jnp.zeros((), BF16)))
                ds = p * (dp - delta_ref[now, h : h + 1, first:last]).astype(BF16)
                part = dot_nn(p, do)
                dv = part if dv is None else jnp.where(lane < low, dv, part)
                part = dot_nn(ds, q)
                dk = part if dk is None else jnp.where(lane < low, dk, part)
                dq.append(dot_nn(kt_ref[now, low:high, :last], ds))
            if ii == 3:
                dkv_ref[now, 0] = dk
                dkv_ref[now, 1] = dv
            else:
                dkv_ref[now, 0, :last, :] += dk
                dkv_ref[now, 1, :last, :] += dv
            dk = dkv_ref[now, 0, first:last, :].astype(BF16)
            dv = dkv_ref[now, 1, first:last, :].astype(BF16)
            dq = (jnp.concatenate(dq, 0) * HEAD_DIM ** -0.5).astype(BF16).T
            dqkv_ref[now, first:last, :width] = dq
            dqkv_ref[now, first:last, width : 2 * width] = dk
            dqkv_ref[now, first:last, 2 * width :] = dv
            bqv_ref[mine, 0:1, :] += jnp.sum(dq.astype(F32), 0, keepdims=True)
            bqv_ref[mine, 1:2, :] += jnp.sum(dv.astype(F32), 0, keepdims=True)

            @pl.when(t >= 8)
            def _():
                da1_ref[first:last, :] += dot_nt(dqkv_ref[now, first:last, :], gq_ref[now])

    serve(1)

    @pl.when((t == 3) | (t == 7) | (t > 13))
    def _():
        @when(3)
        def _():
            fetch.wait()
            fetch_a1t.wait()

        @when(3)
        def _():
            da1_ref[...] = dot_nt(dqkv_ref[now], gq_ref[now])

        @when(7)
        def _():
            da1_ref[...] += dot_nt(dqkv_ref[now], gq_ref[now])

        value = dot_nn(a1t_ref[...], dqkv_ref[now]).reshape(Z_DEV, Y_DEV, depth, 3 * width)
        for s in range(2):
            @when(3 + 11 * s)
            def _():
                if s:
                    core0[0].wait_send()
                stage0_ref[...] = value.astype(BF16)
                start(core0[s])

            @when(7 + 8 * s)
            def _():
                recv(core0[s])
                work0_ref[s] = (value + land0_ref[s].astype(F32)).astype(BF16)
                if s:
                    tail.begin()
                else:
                    start(seg0.y[s])

    @pl.when((t > 8) & (t % 2 == 1))
    def _():
        rows = pl.ds(pl.multiple_of(i * step, step), step)
        xhat, r = norm_parts(own_ref[rows, :].astype(F32))
        da1 = da1_ref[rows, :]
        sums_ref[0, 0:1, :] += jnp.sum(da1 * xhat, 0, keepdims=True)
        sums_ref[0, 2:3, :] += jnp.sum(da1, 0, keepdims=True)
        dg = da1 * rows_ref[0:1, :]
        dv = r * (
            dg
            - jnp.mean(dg, -1, keepdims=True)
            - xhat * jnp.mean(dg * xhat, -1, keepdims=True)
        )
        own_ref[rows, :] = (dh1_ref[...] + dv).astype(BF16)
        for ii in range(4):
            @pl.when(i == ii)
            def _():
                out.send(ii)

    @when(15)
    def _():
        for s in range(4):
            sums_ref[0, 3:5, s * width : (s + 1) * width] = bqv_ref[s, 0:2, :]
        start(sum_core)
        segw.send_x()
        part1_ref[...] = seg1.total()
        part2_ref[...] = seg2.total()
        sent(early_copies)
        tail.fold_high()
        recv(sum_core)
        sums_ref[1] = sums_ref[0] + sumland_ref[0]
        start(sum_y)
        tail.fold_y()
        tail.cross_high()
        tail.fold_z()
        recv(sum_y)
        sums_ref[2] = sums_ref[1] + sumland_ref[1]
        start(sum_z)
        out.pass_on(2)
        tail.finish()
        start(seg0.x)
        recv(sum_z)
        sums_ref[3] = (sums_ref[2] + sumland_ref[2]) + (sumland_ref[3] + sumland_ref[4])
        start(sum_x)
        out.pass_on(1)
        partw_ref[...] = segw.total()
        layer.finish()
        out.pass_on(0)
        recv(sum_x)
        total_ref[...] = sums_ref[3] + sumland_ref[5]
        part0_ref[...] = seg0.total()
        out.finish()
        links.sent(corew[0], core0[0], *early_copies)


def group_and_block(t):
    early = t < 8
    return (
        jnp.where(early, 1 - t // 4, 3 - t % 2),
        3 - jnp.where(early, t % 4, jnp.maximum(t - 8, 0) // 2),
    )


def run_fused_backward(
    tokens, gq, gw, rows, dh1, gb, gbt, q, v, kt, p, scale, o, a1t, layer, fold, work, early
):
    groups, n, _ = tokens.shape
    width = gw.shape[-1]
    heads = width // HEAD_DIM
    hidden = fold.shape[-1]
    depth = D // (Z_DEV * Y_DEV)
    step = n // 4

    p_spec = pl.BlockSpec(
        (1, heads, 1, n, step),
        lambda t: (group_and_block(t)[0], 0, group_and_block(t)[1], 0, 0),
    )

    copies = 12 + 12 + 4 + 15 + 2 * 11 + 8 + 11 + 6

    def landing(lanes, slots=1):
        return [
            pltpu.VMEM((slots, Z_DEV, depth, lanes), BF16),
            pltpu.VMEM((2, 3, depth, lanes), BF16), pltpu.VMEM((2, 2, depth, lanes), BF16),
            pltpu.VMEM((depth, lanes), BF16), pltpu.VMEM((depth, lanes), BF16),
        ]

    def working(lanes):
        block = (Z_DEV, Y_DEV, depth, lanes)
        return [pltpu.VMEM(block, BF16)] + [pltpu.VMEM((2,) + block, BF16)] * 2

    return pl.pallas_call(
        fused_backward,
        grid=(4 * groups,),
        in_specs=[
            ANY_WHOLE, ANY_WHOLE, ANY_WHOLE, VMEM_WHOLE,
            pl.BlockSpec((step, D), lambda t: (group_and_block(jnp.maximum(t, 8))[1], 0)),
            VMEM_WHOLE, ANY_WHOLE, ANY_WHOLE, ANY_WHOLE, ANY_WHOLE, p_spec,
            ANY_WHOLE, ANY_WHOLE, ANY_WHOLE, ANY_WHOLE, ANY_WHOLE, ANY_WHOLE, VMEM_WHOLE,
        ],
        out_specs=[ANY_WHOLE] * 2 + [VMEM_WHOLE] * 5,
        out_shape=[
            shaped(BF16, groups, n, D), shaped(BF16, groups, n, D),
            shaped(F32, depth, 3 * width),
            shaped(F32, depth, width), shaped(F32, depth, hidden),
            shaped(F32, depth, hidden), shaped(F32, 16, D),
        ],
        scratch_shapes=[
            pltpu.VMEM((2, D, 3 * width), BF16), pltpu.VMEM((2, D, width), BF16),
            pltpu.VMEM((2, n, width), BF16), pltpu.VMEM((2, n, width), BF16),
            pltpu.VMEM((2, width, n), BF16), pltpu.VMEM((2, 8, n), F32),
            pltpu.VMEM((2, n, width), BF16),
            pltpu.VMEM((D, n), BF16), pltpu.VMEM((D, n), BF16), pltpu.VMEM((n, D), BF16),
            pltpu.VMEM((2, Z_DEV, depth, hidden), BF16),
            pltpu.VMEM((2, Z_DEV, Y_DEV, depth, hidden), BF16),
            pltpu.VMEM((2, n, width), BF16),
            pltpu.VMEM((2, 8, n), F32), pltpu.VMEM((2, 2, n, width), F32),
            pltpu.VMEM((2, n, 3 * width), BF16), pltpu.VMEM((n, D), F32),
            pltpu.VMEM((n, D), BF16), pltpu.VMEM((n, D), BF16), pltpu.VMEM((n, D), BF16),
            pltpu.VMEM((groups, 8, width), F32),
        ]
        + [pltpu.VMEM((2, Z_DEV, depth, hidden), BF16)] + landing(hidden) + landing(hidden)
        + working(width) + landing(width, 2)
        + working(3 * width) + landing(3 * width)
        + [
            pltpu.VMEM((4, 16, D), F32), pltpu.VMEM((6, 16, D), F32),
            pltpu.SemaphoreType.DMA((copies,)), pltpu.SemaphoreType.DMA((copies,)),
            pltpu.SemaphoreType.DMA((6,)), pltpu.SemaphoreType.DMA((2, 2, 4)),
            pltpu.SemaphoreType.DMA((2, 7)),
            pltpu.VMEM((Z_DEV, depth // 2, 3 * width), BF16),
            pltpu.VMEM((3, depth // 2, 3 * width), BF16),
            pltpu.VMEM((2, depth // 2, 3 * width), BF16),
            pltpu.VMEM((3, Y_DEV, depth // 2, 3 * width), BF16),
            pltpu.VMEM((2, Y_DEV, depth // 2, 3 * width), BF16),
            pltpu.VMEM((Y_DEV, depth // 2, 3 * width), BF16),
            pltpu.VMEM((depth // 2, 3 * width), BF16),
        ],
        compiler_params=pltpu.CompilerParams(
            vmem_limit_bytes=VMEM_LIMIT, collective_id=2, has_side_effects=True
        ),
        name="fused_backward",
    )(tokens, gq, gw, rows, dh1, gb, gbt, q, v, kt, p, scale, o, a1t, layer, fold, work, early)


def place_gradients(
    tie_ref, sums_ref, part0_ref, partw_ref, part1_ref, part2_ref, near_out_ref,
    near_grad_ref, far_out_ref, far_grad_ref, gains_ref, bias_ref, in_ref, out_ref, expand_ref,
    project_ref, chosen_ref,
):
    t = pl.program_id(0)
    far_out_ref[...] = near_out_ref[...]
    far_grad_ref[...] = near_grad_ref[...]
    own = gains_ref.shape[-1]
    width = partw_ref.shape[-1]
    kinds = [tie_ref[0], tie_ref[1], tie_ref[2], tie_ref[3]]

    @pl.when(t == 0)
    def _():
        first = (lax.axis_index("dp") * 4 + lax.axis_index("tensor")) * own
        feature = lax.broadcasted_iota(jnp.int32, (D, 128), 0)
        lane = lax.broadcasted_iota(jnp.int32, (D, 128), 1)
        chosen = ((feature == first + lane) & (lane < own)).astype(F32)
        chosen_ref[...] = lax.dot_general(
            sums_ref[...], chosen, (((1,), (0,)), ((), ())),
            precision=lax.Precision.HIGHEST, preferred_element_type=F32,
        )
        row = lax.broadcasted_iota(jnp.int32, (NSRC, own), 0)
        for i, kind in enumerate([0, 0, 0, 1, 2, 3, 2, 2, 2, 2]):
            value = chosen_ref[2 + i : 3 + i, :own]
            bias_ref[i] = jnp.where(row == kinds[kind], value, 0.0)

    @pl.when(t < NSRC)
    def _():
        def here(kind, value):
            return jnp.where(kinds[kind] == t, value, jnp.zeros_like(value))

        gains_ref[0, 0:1] = here(0, chosen_ref[0:1, :own])
        gains_ref[0, 1:2] = here(2, chosen_ref[1:2, :own])
        for j in range(3):
            in_ref[0, j] = here(0, part0_ref[:, j * width : (j + 1) * width])
        out_ref[0] = here(1, partw_ref[...].T)
        expand_ref[0] = here(2, part1_ref[...])
        project_ref[0] = here(3, part2_ref[...])


def run_place_gradients(tie, sums, part0, partw, part1, part2, out, grad, like):
    slots, n, _ = grad.shape
    gains, biases, w_in, w_out, w_expand, w_project = [item.shape for item in like]
    shapes = [
        gains, (biases[1], biases[0], biases[2]), w_in, w_out, w_expand,
        (w_project[0], w_project[2], w_project[1]),
    ]

    def source(shape):
        return pl.BlockSpec(
            (1,) + shape[1:], lambda t: (jnp.minimum(t, NSRC - 1),) + (0,) * (len(shape) - 1)
        )

    out, grad, gains, biases, w_in, w_out, w_expand, w_project = pl.pallas_call(
        place_gradients,
        grid=(slots,),
        in_specs=[SMEM_WHOLE] + [VMEM_WHOLE] * 5 + [group(n, D), group(n, D)],
        out_specs=[group(n, D), group(n, D), source(shapes[0]), VMEM_WHOLE]
        + [source(shape) for shape in shapes[2:]],
        out_shape=[shaped(BF16, slots, n, D)] * 2 + [shaped(F32, *item) for item in shapes],
        scratch_shapes=[pltpu.VMEM((16, 128), F32)],
        compiler_params=pltpu.CompilerParams(vmem_limit_bytes=VMEM_LIMIT),
        name="place_gradients",
    )(tie, sums, part0, partw, part1, part2, out, grad)
    biases = biases.transpose(1, 0, 2)
    return out, grad, gains, biases, w_in, w_out, w_expand, w_project.transpose(0, 2, 1)


def plain_step(
    tokens, lengths, tie_map, norm_gains, bias_rows, attention_in, attention_out,
    expand_weight, project_weight, cotangent,
):
    slot_rows = tokens.shape[0] // lengths.shape[0]
    me = lax.axis_index("tensor")
    in_local = lax.dynamic_index_in_dim(attention_in, tie_map[0], 0, keepdims=False)
    out_local = lax.dynamic_index_in_dim(attention_out, tie_map[1], 0, keepdims=False)
    expand_local = lax.dynamic_index_in_dim(expand_weight, tie_map[2], 0, keepdims=False)
    project_local = lax.dynamic_index_in_dim(project_weight, tie_map[3], 0, keepdims=False)
    local0 = jnp.concatenate([in_local, out_local.T[None]], 0)
    row_kinds = jnp.array([0, 0, 0, 1, 2, 3] + [2] * (FF // D), dtype=jnp.int32)
    gain_kinds = jnp.array([0, 2], dtype=jnp.int32)
    gain_pick = norm_gains[tie_map[gain_kinds], jnp.arange(2)]
    bias_pick = bias_rows[tie_map[row_kinds], jnp.arange(row_kinds.shape[0])]
    vectors = jnp.concatenate([gain_pick, bias_pick], 0)
    x = lax.dynamic_slice_in_dim(tokens, me * slot_rows, slot_rows, 0)
    cot = lax.dynamic_slice_in_dim(cotangent, me * slot_rows, slot_rows, 0)
    length = lax.dynamic_slice_in_dim(lengths, me, 1, 0)
    rows = lax.all_gather(vectors, ("dp", "tensor"), axis=1, tiled=True).astype(F32)
    rows = jnp.concatenate([rows, jnp.zeros((4, D), F32)], 0)

    def gathered(piece, axis):
        piece = lax.all_gather(piece, "dp", axis=axis, tiled=True)
        return lax.all_gather(piece, "tensor", axis=0)

    g0 = gathered(local0, 1)
    g1 = gathered(expand_local, 0)
    g2 = gathered(project_local.T, 0)
    groups, width = g0.shape[0], g0.shape[-1]
    bqv = rows[3:5].reshape(2, groups, width).transpose(1, 0, 2)
    q, v, kt, p, o, a1t, h1, a2, a2t = run_attention_forward(length, x, g0, rows, bqv)
    out, d1, d2, dh1, gb, gbt, sums = run_feed_forward(length, cot, a2, a2t, h1, g1, g2, rows)
    d0, xg, sums_in, sums_qv = run_attention_backward(
        x, g0, rows, dh1, gb, gbt, q, v, kt, p, o, a1t
    )
    layer_out = lax.all_gather(out, "tensor", axis=0, tiled=True)
    tokens_grad = lax.all_gather(xg, "tensor", axis=0, tiled=True)

    def scattered(piece, axis):
        piece = lax.psum_scatter(piece, "tensor", scatter_dimension=0)
        return lax.psum_scatter(piece, "dp", scatter_dimension=axis, tiled=True).astype(F32)

    part0 = scattered(d0, 1)
    part1 = scattered(d1, 0)
    part2 = scattered(d2, 0)
    qv = sums_qv[:, :2].transpose(1, 0, 2).reshape(2, D)
    sums = jnp.concatenate(
        [sums_in[0:1], sums[1:2], sums_in[1:2], qv, sums[5:12]], 0
    )
    sums = lax.psum_scatter(sums, ("dp", "tensor"), scatter_dimension=1, tiled=True)
    return layer_out, tokens_grad, *placed(tie_map, sums, part0, part1, part2)


def fused_step(
    tokens, lengths, tie_map, norm_gains, bias_rows, attention_in, attention_out,
    expand_weight, project_weight, cotangent,
):
    slots = lengths.shape[0]
    tokens = tokens.reshape(slots, -1, D)
    cotangent = cotangent.reshape(slots, -1, D)
    gq, gw, g1, g2, rows, q, v, kt, p, scale, o, a1t, h1, a2, a2t = run_fused_forward(
        tie_map, lengths, tokens, norm_gains, bias_rows, attention_in, attention_out,
        expand_weight, project_weight,
    )
    layer, fold, work, dh1, gb, gbt, early = run_fused_feed_forward(
        lengths, cotangent, a2, a2t, h1, g1, g2, rows
    )
    grad, out, part0, partw, part1, part2, sums = run_fused_backward(
        tokens, gq, gw, rows, dh1, gb, gbt, q, v, kt, p, scale, o, a1t, layer, fold,
        work, early,
    )
    out, grad, *placed_grads = run_place_gradients(
        tie_map, sums, part0, partw, part1, part2, out, grad,
        (norm_gains, bias_rows, attention_in, attention_out, expand_weight, project_weight),
    )
    return out.reshape(-1, D), grad.reshape(-1, D), *placed_grads


def placed(tie_map, sums, part0, part1, part2):
    source = jnp.arange(NSRC, dtype=jnp.int32)

    def place(piece, which):
        pick = (source == tie_map[which]).reshape((NSRC,) + (1,) * piece.ndim)
        return jnp.where(pick, piece[None], 0.0)

    def place_rows(piece, kinds):
        pick = source[:, None] == tie_map[jnp.array(kinds, dtype=jnp.int32)][None, :]
        return jnp.where(pick[:, :, None], piece[None], 0.0)

    return (
        place_rows(sums[:2], [0, 2]),
        place_rows(sums[2:], [0, 0, 0, 1, 2, 3] + [2] * (FF // D)),
        place(part0[:3], 0),
        place(part0[3].T, 1),
        place(part1, 2),
        place(part2.T, 3),
    )


def solution(mesh):
    fused = mesh.shape["dp"] == Z_DEV * Y_DEV and mesh.shape["tensor"] == X_DEV * C_DEV
    return jax.shard_map(
        fused_step if fused else plain_step,
        mesh=mesh,
        in_specs=(
            P("dp", None),
            P("dp"),
            P(),
            P(None, None, ("dp", "tensor")),
            P(None, None, ("dp", "tensor")),
            P(None, None, "dp", "tensor"),
            P(None, "tensor", "dp"),
            P(None, "dp", "tensor"),
            P(None, "tensor", "dp"),
            P("dp", None),
        ),
        out_specs=(
            P("dp", None),
            P("dp", None),
            P(None, None, ("dp", "tensor")),
            P(None, None, ("dp", "tensor")),
            P(None, None, "dp", "tensor"),
            P(None, "tensor", "dp"),
            P(None, "dp", "tensor"),
            P(None, "tensor", "dp"),
        ),
        check_vma=False,
    )
```
